32 devices in a mesh: batch: 4 (over y, x), neuron: 8 (over z, core).
Axes of the slice: x: 2, y: 2, z: 4, core: 2. Of those that a mesh axis runs over, the one named last changes fastest.
Arguments:
- inputs: float32 [2048, 5120], P('neuron', 'batch'), may hold values from -19 to 19
- weights: float32 [2, 2048, 2048], P(None, 'neuron'), may hold values from -0.1875 to 0.1875
- gains: float32 [2, 2048], P(None, 'neuron'), may hold values from 0.5 to 1.5
- shifts: float32 [2, 2048], P(None, 'neuron'), may hold values from -3 to 3
- decays: float32 [2, 2048], P(None, 'neuron'), may hold values from 0.1 to 0.95
- biases: float32 [2, 2048], P(None, 'neuron'), may hold values from -3 to 3
- lengths: int32 [16], P('batch'), may hold values from 21 to 320, as said below
- frame_mask: int32 [16, 320], P('batch'), may hold values 0 or 1
- grad_out: float32 [2048, 5120], P('neuron', 'batch'), may hold values from -6 to 6
Outputs:
- output: float32 [2048, 5120], P('neuron', 'batch')
- grad_in: float32 [2048, 5120], P('neuron', 'batch')
- grad_weights: float32 [2, 2048, 2048], P(None, 'neuron')
- grad_gains: float32 [2, 2048], P(None, 'neuron')
- grad_shifts: float32 [2, 2048], P(None, 'neuron')
- grad_decays: float32 [2, 2048], P(None, 'neuron')
- grad_biases: float32 [2, 2048], P(None, 'neuron')
The draws below stay inside these ranges and needn't reach their ends.
Inputs may be any that keep to these rules, and one draw needn't show every extreme that they name: `lengths`: some clip has exactly 320 frames.
All inputs are finite; a program needn't handle non-finite values. No bound on the sum of `frame_mask` on one device may be relied on, other than what follows from the above.
Results may differ from the reference program's by a relative error of at most 0.0003.
Values sent between devices are 32-bit elements; how exact they have to be, the bound alone decides.
No kernel may reach another device: no remote copies, remote signals or barrier semaphores. Data moves between devices by JAX's collectives and lax.ppermute only.
A program may use at most 128 MiB of HBM per device.

```python
import jax
import jax.numpy as jnp
from jax import lax

H = 2048
LAYERS = 2
LMAX = 320
CLIPS = 16


def draw_inputs(key, part):
    key = jax.random.fold_in(key, 11)
    base_key, jitter_key, offset_key = jax.random.split(key, 3)
    ramp = 3.0 ** (jnp.arange(CLIPS, dtype=jnp.float32) / max(CLIPS - 1, 1))
    jitter = jax.random.uniform(jitter_key, (CLIPS,), jnp.float32, 0.8, 1.25)
    scales = jnp.repeat(0.6 * ramp * jitter, LMAX)
    offset = 0.7 * jnp.clip(jax.random.normal(offset_key, (H,), jnp.float32), -3.0, 3.0)
    base = jnp.clip(jax.random.normal(base_key, (H, CLIPS * LMAX), jnp.float32), -6.0, 6.0)
    return (scales[None, :] * (base + offset[:, None])).astype(jnp.float32)


def draw_lengths(key, part):
    key = jax.random.fold_in(key, 23)
    pick_key, length_key = jax.random.split(key)
    drawn = jax.random.randint(length_key, (CLIPS,), LMAX // 15, LMAX + 1, jnp.int32)
    longest = jax.random.randint(pick_key, (), 0, CLIPS, jnp.int32)
    return jnp.where(jnp.arange(CLIPS, dtype=jnp.int32) == longest, LMAX, drawn).astype(jnp.int32)


def touch_ends(array, rng, smallest, top_value):
    longest = array.shape.index(max(array.shape))
    spots = []
    for shift in (0, 1):
        where = [jax.random.randint(jax.random.fold_in(rng, axis), (), 0, length) for axis, length in enumerate(array.shape)]
        where[longest] = (where[longest] + shift) % array.shape[longest]
        spots.append(tuple(where))
    return array.at[spots[0]].set(smallest).at[spots[1]].set(top_value)


def with_spikes(values, stream_key, source, target, blocks, factor):
    def block_of(dim):
        return (jnp.arange(values.shape[dim]) // (values.shape[dim] // blocks)).reshape((-1,) + (1,) * (values.ndim - 1 - dim))

    one_side = jax.random.permutation(stream_key, blocks)[block_of(target)]
    second = (block_of(target) + blocks // 2) % blocks
    return jnp.where((block_of(source) == one_side) | (block_of(source) == second), factor * values, values)


def level_of(stream_key, extent, cuts, smallest, top_value):
    def one(dim, shards_of):
        draws = jax.random.uniform(jax.random.fold_in(jax.random.fold_in(stream_key, 6), dim), (shards_of,), jnp.float32, smallest / len(cuts), top_value / len(cuts))
        return jnp.repeat(jnp.exp(draws), extent[dim] // shards_of).reshape((-1,) + (1,) * (len(extent) - dim - 1))

    loudness = one(*cuts[0])
    for cut in cuts[1:]:
        loudness = loudness * one(*cut)
    return loudness


def noise(stream_key, dims, deviation, limit, cuts=(), held_as=jnp.bfloat16):
    values = deviation * jax.random.normal(stream_key, dims, jnp.float32)
    if cuts:
        values = values * level_of(stream_key, dims, cuts, -0.22, 0.18)
    return jnp.clip(values, -limit, limit).astype(held_as)


def bell_draw_with(rng, shape, scale, most, cuts, heavy, held_as=jnp.bfloat16):
    array = scale * jax.random.normal(rng, shape, jnp.float32)
    if cuts:
        array = array * level_of(rng, shape, cuts, -0.22, 0.18)
    return jnp.clip(with_spikes(array, jax.random.fold_in(rng, 3), *heavy), -most, most).astype(held_as)


def setup_inputs(seed: int = 0) -> dict:
    streams_of = jax.random.split(jax.random.key(seed), 10)
    return {
        "inputs": draw_inputs(jax.random.fold_in(streams_of[9], 71), 0),
        "weights": bell_draw_with(streams_of[1], (LAYERS, H, H), H ** -0.5, 0.1875, ((1, 8),), (1, 2, 8, 2.0), jnp.float32),
        "gains": jnp.clip(1.0 + 0.1 * jax.random.normal(streams_of[2], (LAYERS, H), jnp.float32), 0.5, 1.5),
        "shifts": noise(streams_of[3], (LAYERS, H), 0.5, 3.0, ((1, 8),), jnp.float32),
        "decays": jnp.clip(0.1 + 0.84999999 * jax.random.uniform(streams_of[4], (LAYERS, H), jnp.float32) ** level_of(streams_of[4], (LAYERS, H), ((1, 8),), -0.2, 0.2), 0.1, 0.95),
        "biases": noise(streams_of[5], (LAYERS, H), 0.5, 3.0, ((1, 8),), jnp.float32),
        "lengths": draw_lengths(jax.random.fold_in(streams_of[9], 71), 0),
        "frame_mask": touch_ends((jax.random.randint(streams_of[7], (CLIPS, LMAX), 0, 8) < 7).astype(jnp.int32), jax.random.fold_in(streams_of[7], 1), 0, 1),
        "grad_out": noise(streams_of[8], (H, CLIPS * LMAX), 1.0, 6.0, ((0, 8), (1, 4)), jnp.float32),
    }


@jax.custom_vjp
def low(v):
    return lax.optimization_barrier(v.astype(jnp.bfloat16)).astype(jnp.float32)

@jax.custom_vjp
def low_back(v):
    return v

def low_keep(v):
    return (low(v), None)

def low_pass(kept, grad):
    return (grad,)

def back_keep(v):
    return (v, None)

def back_low(kept, grad):
    return (low(grad),)
low.defvjp(low_keep, low_pass)
low_back.defvjp(back_keep, back_low)
EPS = 1e-05
HIGH = lax.Precision.HIGHEST

def recur_step(decay, state, inputs):
    drive_t, valid_t = inputs
    pre = drive_t + decay * state
    state = state + valid_t[None, :] * (jax.nn.gelu(pre, approximate=False) - state)
    return (state, state)

def one_layer(layer_in, weight, gain, shift, decay, bias, valid, count):
    width, slots = layer_in.shape
    pre_norm = jnp.dot(weight, layer_in, precision=HIGH, preferred_element_type=jnp.float32)
    mean = lax.optimization_barrier(jnp.sum(valid[None, :] * pre_norm, axis=1)) / count
    centered = pre_norm - mean[:, None]
    var = lax.optimization_barrier(jnp.sum(valid[None, :] * centered * centered, axis=1)) / count
    drive = gain[:, None] * centered * lax.rsqrt(var + EPS)[:, None] + (shift + bias)[:, None]
    drive_time = jnp.transpose(drive.reshape(width, CLIPS, LMAX), (2, 0, 1))
    valid_time = valid.reshape(CLIPS, LMAX).T
    step_fn = jax.checkpoint(lambda state, inputs: recur_step(decay[:, None], state, inputs))
    start = jnp.zeros((width, CLIPS), jnp.float32)
    _, states = lax.scan(step_fn, start, (drive_time, valid_time))
    states_flat = jnp.transpose(states, (1, 2, 0)).reshape(width, slots)
    return layer_in + valid[None, :] * states_flat

def reference(inputs, weights, gains, shifts, decays, biases, lengths, frame_mask, grad_out):
    frames = jnp.arange(LMAX, dtype=jnp.int32)
    valid = ((frames[None, :] < lengths[:, None]) & ((frame_mask == 1) | (frames[None, :] == 0))).astype(jnp.float32).reshape(-1)
    count = jnp.sum(valid)

    def forward(inputs, weights, gains, shifts, decays, biases):
        layer_in = inputs
        for layer_no in range(LAYERS):
            layer_in = one_layer(layer_in, weights[layer_no], gains[layer_no], shifts[layer_no], decays[layer_no], biases[layer_no], valid, count)
        return layer_in
    output, pullback = jax.vjp(forward, inputs, weights, gains, shifts, decays, biases)
    grad_in, grad_weights, grad_gains, grad_shifts, grad_decays, grad_biases = pullback(grad_out)
    return (output, grad_in, grad_weights, grad_gains, grad_shifts, grad_decays, grad_biases)
```

```python
from functools import partial
import math

import jax
import jax.numpy as jnp
from jax import lax
from jax.experimental import pallas as pl
from jax.experimental.pallas import tpu as pltpu
from jax.sharding import Mesh, PartitionSpec as P

LAYERS = 2
EPS = 1e-05
HIGH = lax.Precision.HIGHEST
ROOT_TWO = math.sqrt(2.0)
ROOT_TWO_PI = math.sqrt(2.0 * math.pi)
F32 = jnp.float32
BF16 = jnp.bfloat16
LANES = 128
VMEM_LIMIT = 48 * 1024 * 1024
SMEM_SPEC = pl.BlockSpec(memory_space=pltpu.SMEM)
VMEM_SPEC = pl.BlockSpec(memory_space=pltpu.VMEM)


FLIP2 = [(0, 1), (1, 0)]


def flip_of(rel):
    if rel == 1:
        return "c", FLIP2
    if rel == 2:
        return "h", FLIP2
    return ("h", "c"), [(i, i ^ 3) for i in range(4)]


def swap(array, rel):
    if rel == 0:
        return array
    axes, pairs = flip_of(rel)
    return lax.ppermute(array, axes, pairs)


def swap_half(array):
    return lax.ppermute(array, "l", FLIP2)


def split(value):
    high = value.astype(BF16)
    return high, (value - high.astype(F32)).astype(BF16)


def dot(a, b, dims):
    return lax.dot_general(a, b, (dims, ((), ())), preferred_element_type=F32)


NT = ((1,), (1,))
NN = ((1,), (0,))


def call(body, **kwargs):
    return pl.pallas_call(
        body,
        compiler_params=pltpu.CompilerParams(vmem_limit_bytes=VMEM_LIMIT),
        **kwargs,
    )


def cost(flops, byte_count):
    return pl.CostEstimate(flops=int(flops) // 64, bytes_accessed=int(byte_count) // 64, transcendentals=0)


def pack_body(frames, place_ref, in_ref, *refs):
    outs, turned = refs[:4], refs[4]
    slots = in_ref.shape[1]
    for start in range(0, slots, LANES):
        turned[start : start + LANES, :] = in_ref[:, start : start + LANES].T
    for rel in range(4):
        first = pl.multiple_of(place_ref[rel] * frames, 8)
        outs[rel][...] = turned[pl.ds(first, frames), :]


def pack(place, array, frames):
    width, slots = array.shape
    return call(
        partial(pack_body, frames),
        out_shape=[jax.ShapeDtypeStruct((frames, width), F32)] * 4,
        in_specs=[SMEM_SPEC, VMEM_SPEC],
        out_specs=[VMEM_SPEC] * 4,
        scratch_shapes=[pltpu.VMEM((slots, width), F32)],
        cost_estimate=cost(0, 8 * width * slots),
        name="pack",
    )(place, array)


def unpack_body(frames, place_ref, *refs):
    ins, out_ref, turned = refs[:4], refs[4], refs[5]
    slots = out_ref.shape[1]
    for rel in range(4):
        first = pl.multiple_of(place_ref[rel] * frames, 8)
        turned[pl.ds(first, frames), :] = ins[rel][...]
    for start in range(0, slots, LANES):
        out_ref[:, start : start + LANES] = turned[start : start + LANES, :].T


def unpack(place, pieces):
    frames, width = pieces[0].shape
    slots = 4 * frames
    return call(
        partial(unpack_body, frames),
        out_shape=jax.ShapeDtypeStruct((width, slots), F32),
        in_specs=[SMEM_SPEC] + [VMEM_SPEC] * 4,
        out_specs=VMEM_SPEC,
        scratch_shapes=[pltpu.VMEM((slots, width), F32)],
        cost_estimate=cost(0, 8 * width * slots),
        name="unpack",
    )(place, *pieces)


def spread_of(parts, width):
    spots, row, column = [], 0, 0
    for part in parts:
        spots.append((row, column))
        if part.shape[1] == width:
            column += width
        else:
            row += part.shape[0]
    return spots


def put_split(spots, part_refs, high_ref, low_ref):
    width = high_ref.shape[2]
    for (row, column), part in zip(spots, part_refs):
        rows, columns = part.shape
        for start in range(0, columns, width):
            block = (column + start) // width
            high, low = split(part[:, start : start + width])
            high_ref[block, row : row + rows, :] = high
            low_ref[block, row : row + rows, :] = low


def project_body(n_parts, spots, with_acc, with_stats, cols_ref, place_ref, *refs):
    del cols_ref
    parts, refs = refs[:n_parts], refs[n_parts:]
    weights, refs = refs[:4], refs[4:]
    if with_acc:
        acc_ref, refs = refs[0], refs[1:]
    if with_stats:
        valid_ref, refs = refs[0], refs[1:]
        out_ref, stats_ref, x_high, x_low = refs
    else:
        out_ref, x_high, x_low = refs
    step = pl.program_id(0)
    width = x_high.shape[2]

    @pl.when(step == 0)
    def _():
        put_split(spots, parts, x_high, x_low)
        if with_acc:
            out_ref[...] = acc_ref[...]
        else:
            out_ref[...] = jnp.zeros_like(out_ref)

    stacked = jnp.concatenate([x_high[step], x_low[step], x_high[step]], axis=1)
    for block in range(4):
        w_high, w_low = split(weights[block][...].reshape(width, width))
        columns = slice(block * width, (block + 1) * width)
        out_ref[:, columns] += dot(stacked, jnp.concatenate([w_high, w_high, w_low], axis=1), NT)

    if with_stats:

        @pl.when(step == pl.num_programs(0) - 1)
        def _():
            valid = valid_ref[...]
            own = jnp.sum(valid, axis=0, keepdims=True)
            for row in range(out_ref.shape[1] // LANES):
                z = out_ref[:, row * LANES : (row + 1) * LANES]
                total = jnp.sum(valid * z, axis=0, keepdims=True)
                centred = valid * (z - total / own)
                squares = jnp.sum(centred * centred, axis=0, keepdims=True)
                per = width // LANES
                at = place_ref[row // per] * per + row % per
                stats_ref[0, pl.ds(at, 1), :] = total
                stats_ref[1, pl.ds(at, 1), :] = squares
                stats_ref[2, pl.ds(at, 1), :] = own


def weight_specs(weights, layer):
    specs = []
    for weight in weights:
        width = weight.shape[-2]
        if weight.ndim == 3:
            specs.append(pl.BlockSpec((1, width, width), lambda s, cols, *_: (layer, 0, cols[s])))
        else:
            specs.append(pl.BlockSpec((width, width), lambda s, cols, *_: (0, cols[s])))
    return specs


def project(columns, place, parts, weights, layer, acc=None, valid=None):
    width = weights[0].shape[-2]
    frames = sum(p.shape[0] for p in parts if p.shape[1] != width) or parts[0].shape[0]
    full = pl.BlockSpec(memory_space=pltpu.VMEM)
    in_specs = [full] * len(parts)
    in_specs += weight_specs(weights, layer)
    operands = list(parts) + list(weights)
    out_shape = [jax.ShapeDtypeStruct((frames, 4 * width), F32)]
    out_specs = [pl.BlockSpec((frames, 4 * width), lambda s, cols, place: (0, 0))]
    if acc is not None:
        in_specs.append(full)
        operands.append(acc)
    if valid is not None:
        in_specs.append(full)
        operands.append(valid)
        rows = 4 * width // LANES
        out_shape.append(jax.ShapeDtypeStruct((3, rows, LANES), F32))
        out_specs.append(pl.BlockSpec((3, rows, LANES), lambda s, cols, place: (0, 0, 0)))
    return call(
        partial(
            project_body, len(parts), spread_of(parts, width), acc is not None, valid is not None
        ),
        grid_spec=pltpu.PrefetchScalarGridSpec(
            num_scalar_prefetch=2,
            grid=(4,),
            in_specs=in_specs,
            out_specs=out_specs,
            scratch_shapes=[pltpu.VMEM((4, frames, width), BF16)] * 2,
        ),
        out_shape=out_shape,
        cost_estimate=cost(2 * 3 * frames * 16 * width * width, 4 * 16 * width * width),
        name="project",
    )(columns, place, *operands)


def to_relative(place_ref, spread, rows_ref, value, slot):
    per = value.shape[0] // 4
    spread[...] = value
    for rel in range(4):
        first = place_ref[rel] * per
        for row in range(per):
            rows_ref[slot, rel * per + row : rel * per + row + 1, :] = spread[
                pl.ds(first + row, 1), :
            ]


def norm_terms(stats_ref):
    devices = stats_ref.shape[0]
    count = stats_ref[0, 2]
    total = stats_ref[0, 0]
    for i in range(1, devices):
        count = count + stats_ref[i, 2]
        total = total + stats_ref[i, 0]
    mean = total / count
    squares = jnp.zeros_like(mean)
    for i in range(devices):
        away = stats_ref[i, 0] / stats_ref[i, 2] - mean
        squares = squares + (stats_ref[i, 1] + stats_ref[i, 2] * away * away)
    return count, mean, lax.rsqrt(squares / count + EPS)


def recur_body(n_parts, spots, out_cols, first, width, place_ref, gate_ref, z_ref, stats_ref, params_ref, valid_ref, start_ref, *refs):
    parts, refs = refs[:n_parts], refs[n_parts:]
    n_out = len(out_cols)
    outs, refs = refs[:n_out], refs[n_out:]
    state_ref, slope_ref, last_ref, rows, spread, drive_s, state_s, slope_s = refs
    frames = z_ref.shape[0]
    blocks = z_ref.shape[1] // LANES
    _, mean, inv_std = norm_terms(stats_ref)
    to_relative(place_ref, spread, rows, mean, 0)
    to_relative(place_ref, spread, rows, params_ref[0] * inv_std, 1)
    to_relative(place_ref, spread, rows, params_ref[1], 2)
    to_relative(place_ref, spread, rows, params_ref[2], 3)
    for row in range(blocks):
        z = z_ref[:, row * LANES : (row + 1) * LANES]
        drive_s[row * frames : (row + 1) * frames, :] = (
            z - rows[0, row : row + 1, :]
        ) * rows[1, row : row + 1, :] + rows[2, row : row + 1, :]
    decay = rows[3]

    def step(t, state):
        at = pl.ds(t, blocks, stride=frames)
        pre = drive_s[at, :] + decay * state
        half = 0.5 + 0.5 * lax.erf(pre * (1.0 / ROOT_TWO))
        gate = gate_ref[first + t] > 0.0
        slope = half + pre * jnp.exp(-0.5 * pre * pre) * (1.0 / ROOT_TWO_PI)
        state = jnp.where(gate, pre * half, state)
        state_s[at, :] = state
        slope_s[at, :] = jnp.where(gate, slope, 0.0)
        return state

    last_ref[...] = lax.fori_loop(0, frames, step, start_ref[...], unroll=8)
    valid = valid_ref[...]
    for row in range(blocks):
        lanes = slice(row * LANES, (row + 1) * LANES)
        state = state_s[row * frames : (row + 1) * frames, :]
        state_ref[:, lanes] = state
        slope_ref[:, lanes] = slope_s[row * frames : (row + 1) * frames, :]
        for (_, column), part in zip(spots, parts):
            if column <= row * LANES < column + part.shape[1]:
                x = part[:, row * LANES - column : (row + 1) * LANES - column]
        for column, out in zip(out_cols, outs):
            if column <= row * LANES < column + out.shape[1]:
                out[:, row * LANES - column : (row + 1) * LANES - column] = x + valid * state


def recur(chunk, chunks, place, gate, z, stats, params, valid, start, parts, pieces):
    frames = z.shape[0] // chunks
    features = z.shape[1]
    width = features // 4
    blocks = features // LANES
    row_block = lambda columns: pl.BlockSpec((frames, columns), lambda i: (chunk, 0))
    whole = lambda array: pl.BlockSpec(array.shape, lambda i: (0,) * array.ndim)
    part_specs = [row_block(p.shape[1]) if p.shape[0] == z.shape[0] else whole(p) for p in parts]
    n_out = pieces
    out_width = features // n_out
    tile = jax.ShapeDtypeStruct((blocks, LANES), F32)
    full = jax.ShapeDtypeStruct((frames, features), F32)
    out_shape = [jax.ShapeDtypeStruct((frames, out_width), F32)] * n_out + [full, full, tile]
    return call(
        partial(
            recur_body,
            len(parts),
            spread_of(parts, width),
            [i * out_width for i in range(n_out)],
            chunk * frames,
            width,
        ),
        grid=(1,),
        in_specs=[
            SMEM_SPEC,
            SMEM_SPEC,
            row_block(features),
            whole(stats),
            whole(params),
            row_block(LANES),
            whole(start),
        ]
        + part_specs,
        out_specs=[whole(s) for s in out_shape],
        out_shape=out_shape,
        scratch_shapes=[
            pltpu.VMEM((4, blocks, LANES), F32),
            pltpu.VMEM((blocks, LANES), F32),
        ]
        + [pltpu.VMEM((blocks * frames, LANES), F32)] * 3,
        cost_estimate=cost(100 * frames * features, 20 * frames * features),
        name="recur",
    )(place, gate, z, stats, params, valid, start, *parts)


def back_body(n_parts, spots, n_state, place_ref, gate_ref, z_ref, stats_ref, params_ref, *refs):
    parts, refs = refs[:n_parts], refs[n_parts:]
    states, refs = refs[:n_state], refs[n_state:]
    slopes, refs = refs[:n_state], refs[n_state:]
    grad_ref, sums_ref, rows, spread, up_s, zhat_s, state_s, slope_s = refs
    frames = z_ref.shape[0]
    blocks = z_ref.shape[1] // LANES
    tall = frames + 8
    _, mean, inv_std = norm_terms(stats_ref)
    to_relative(place_ref, spread, rows, mean, 0)
    to_relative(place_ref, spread, rows, inv_std, 1)
    to_relative(place_ref, spread, rows, params_ref[2], 2)
    for row in range(blocks):
        lanes = slice(row * LANES, (row + 1) * LANES)
        base = row * frames
        zhat_s[base : base + frames, :] = (z_ref[:, lanes] - rows[0, row : row + 1, :]) * rows[
            1, row : row + 1, :
        ]
        up = None
        for (top, column), part in zip(spots, parts):
            if column <= row * LANES < column + part.shape[1] and part.shape[0] == frames:
                value = part[:, row * LANES - column : (row + 1) * LANES - column]
                up = value if up is None else up + value
        up_s[base : base + frames, :] = up
        state_s[row * tall : row * tall + 8, :] = jnp.zeros((8, LANES), F32)
        first = 0
        for state, slope in zip(states, slopes):
            some = state.shape[0]
            at = row * tall + 8 + first
            state_s[at : at + some, :] = state[:, lanes]
            slope_s[base + first : base + first + some, :] = slope[:, lanes]
            first += some
    decay = rows[2]
    zero = jnp.zeros((blocks, LANES), F32)

    def step(i, carried):
        carry, sum_gain, sum_shift, sum_decay = carried
        t = frames - 1 - i
        at = pl.ds(t, blocks, stride=frames)
        slope = slope_s[at, :]
        keep = 1.0 - gate_ref[t]
        total = gate_ref[t] * up_s[at, :] + carry
        grad = total * slope
        carry = total * (slope * decay + keep)
        up_s[at, :] = grad
        sum_gain = sum_gain + grad * zhat_s[at, :]
        sum_shift = sum_shift + grad
        sum_decay = sum_decay + grad * state_s[pl.ds(t + 7, blocks, stride=tall), :]
        return carry, sum_gain, sum_shift, sum_decay

    _, sum_gain, sum_shift, sum_decay = lax.fori_loop(
        0, frames, step, (zero, zero, zero, zero), unroll=8
    )
    for row in range(blocks):
        grad_ref[:, row * LANES : (row + 1) * LANES] = up_s[row * frames : (row + 1) * frames, :]
    per = blocks // 4
    for slot, value in enumerate((sum_gain, sum_shift, sum_decay)):
        spread[...] = value
        for rel in range(4):
            for row in range(per):
                sums_ref[slot, pl.ds(place_ref[rel] * per + row, 1), :] = spread[
                    rel * per + row : rel * per + row + 1, :
                ]


def spots_of_sum(parts, width):
    spots, column = [], 0
    for part in parts:
        if part.shape[1] == width:
            spots.append((0, column))
            column += width
        else:
            spots.append((0, 0))
    return spots


def back(place, gate, z, stats, params, ups, states, slopes):
    frames, features = z.shape
    width = features // 4
    blocks = features // LANES
    return call(
        partial(back_body, len(ups), spots_of_sum(ups, width), len(states)),
        in_specs=[SMEM_SPEC] * 2 + [VMEM_SPEC] * (3 + len(ups) + 2 * len(states)),
        out_specs=[VMEM_SPEC] * 2,
        out_shape=[
            jax.ShapeDtypeStruct((frames, features), F32),
            jax.ShapeDtypeStruct((3, blocks, LANES), F32),
        ],
        scratch_shapes=[
            pltpu.VMEM((3, blocks, LANES), F32),
            pltpu.VMEM((blocks, LANES), F32),
            pltpu.VMEM((blocks * frames, LANES), F32),
            pltpu.VMEM((blocks * frames, LANES), F32),
            pltpu.VMEM((blocks * (frames + 8), LANES), F32),
            pltpu.VMEM((blocks * frames, LANES), F32),
        ],
        cost_estimate=cost(30 * frames * features, 20 * frames * features),
        name="back",
    )(place, gate, z, stats, params, *ups, *states, *slopes)


def input_terms(high_s, low_s, weights):
    width = high_s.shape[2]
    left, right = [], []
    for block, weight in enumerate(weights):
        w_high, w_low = split(weight[...].reshape(width, width))
        left += [high_s[block], low_s[block], high_s[block]]
        right += [w_high, w_high, w_low]
    return dot(jnp.concatenate(left, axis=1), jnp.concatenate(right, axis=0), NN)


def norm_back_body(cols_ref, place_ref, grad_ref, z_ref, stats_ref, params_ref, sums_ref, valid_ref, w0, w1, w2, w3, out_ref, term_ref, sums_out_ref, rows, spread, high_s, low_s):
    del cols_ref
    blocks = z_ref.shape[1] // LANES
    width = high_s.shape[2]
    per = width // LANES

    @pl.when(pl.program_id(0) == 0)
    def _():
        count, mean, inv_std = norm_terms(stats_ref)
        to_relative(place_ref, spread, rows, mean, 0)
        to_relative(place_ref, spread, rows, inv_std, 1)
        to_relative(place_ref, spread, rows, params_ref[0] * inv_std, 2)
        sums = sums_ref[0]
        for i in range(1, sums_ref.shape[0]):
            sums = sums + sums_ref[i]
        sums_out_ref[...] = sums
        to_relative(place_ref, spread, rows, sums[0] / count, 3)
        to_relative(place_ref, spread, rows, sums[1] / count, 4)
        valid = valid_ref[...]
        for row in range(blocks):
            lanes = slice(row * LANES, (row + 1) * LANES)
            one = lambda slot: rows[slot, row : row + 1, :]
            zhat = (z_ref[:, lanes] - one(0)) * one(1)
            value = one(2) * (grad_ref[:, lanes] - valid * (one(4) + zhat * one(3)))
            out_ref[:, lanes] = value
            high, low = split(value)
            inner = slice((row % per) * LANES, (row % per + 1) * LANES)
            high_s[row // per, :, inner] = high
            low_s[row // per, :, inner] = low

    term_ref[...] = input_terms(high_s, low_s, (w0, w1, w2, w3))


def norm_back(columns, place, grad, z, stats, params, sums, valid, weights, layer):
    frames, features = z.shape
    width = features // 4
    blocks = features // LANES
    whole = lambda array: pl.BlockSpec(array.shape, lambda s, cols, place: (0,) * array.ndim)
    operands = [grad, z, stats, params, sums, valid]
    full = jax.ShapeDtypeStruct((frames, features), F32)
    return call(
        norm_back_body,
        grid_spec=pltpu.PrefetchScalarGridSpec(
            num_scalar_prefetch=2,
            grid=(4,),
            in_specs=[whole(a) for a in operands] + weight_specs(weights, layer),
            out_specs=[
                whole(full),
                pl.BlockSpec((frames, width), lambda s, cols, place: (0, s)),
                pl.BlockSpec((3, blocks, LANES), lambda s, cols, place: (0, 0, 0)),
            ],
            scratch_shapes=[
                pltpu.VMEM((5, blocks, LANES), F32),
                pltpu.VMEM((blocks, LANES), F32),
                pltpu.VMEM((4, frames, width), BF16),
                pltpu.VMEM((4, frames, width), BF16),
            ],
        ),
        out_shape=[full, full, jax.ShapeDtypeStruct((3, blocks, LANES), F32)],
        cost_estimate=cost(6 * frames * features * features, 4 * features * features),
        name="norm_back",
    )(columns, place, *operands, *weights)


def own_terms_body(n_ups, piecewise, cols_ref, grad_ref, *refs):
    del cols_ref
    ups, refs = refs[:n_ups], refs[n_ups:]
    weights, refs = refs[:4], refs[4:]
    out_ref, high_s, low_s = refs
    width = high_s.shape[2]
    step = pl.program_id(0)

    @pl.when(step == 0)
    def _():
        for block in range(4):
            high, low = split(grad_ref[:, block * width : (block + 1) * width])
            high_s[block] = high
            low_s[block] = low

    total = input_terms(high_s, low_s, weights)
    if piecewise:
        for block in range(4):

            @pl.when(step == block)
            def _():
                out_ref[...] = total + ups[block][...]
    else:
        for up in ups:
            total = total + up[...]
        out_ref[...] = total


def own_terms(columns, grad, ups, weights, layer):
    frames, features = grad.shape
    width = features // 4
    piecewise = ups[0].shape[1] == width
    whole = lambda array: pl.BlockSpec(array.shape, lambda s, cols: (0,) * array.ndim)
    step_block = pl.BlockSpec((frames, width), lambda s, cols: (0, s))
    return call(
        partial(own_terms_body, len(ups), piecewise),
        grid_spec=pltpu.PrefetchScalarGridSpec(
            num_scalar_prefetch=1,
            grid=(4,),
            in_specs=[whole(grad)]
            + [whole(u) if piecewise else step_block for u in ups]
            + weight_specs(weights, layer),
            out_specs=step_block,
            scratch_shapes=[pltpu.VMEM((4, frames, width), BF16)] * 2,
        ),
        out_shape=jax.ShapeDtypeStruct((frames, features), F32),
        cost_estimate=cost(6 * frames * features * features, 4 * features * features),
        name="own_terms",
    )(columns, grad, *ups, *weights)


def weight_body(n_parts, spots_own, spots_other, rels, from_ref, grad_ref, *refs):
    own, refs = refs[:n_parts], refs[n_parts:]
    other, refs = refs[:n_parts], refs[n_parts:]
    added, refs = refs[:-3], refs[-3:]
    out_ref, turned, x_all = refs
    step = pl.program_id(0)
    width = x_all.shape[2]
    frames = grad_ref.shape[0]

    @pl.when(step == 0)
    def _():
        for first, spots, parts in ((0, spots_own, own), (4, spots_other, other)):
            for (row, column), part in zip(spots, parts):
                rows, columns = part.shape
                for start in range(0, columns, width):
                    block = first + (column + start) // width
                    high, low = split(part[:, start : start + width])
                    x_all[block, row : row + rows, :] = high
                    x_all[block, frames + row : frames + row + rows, :] = low
                    x_all[block, 2 * frames + row : 2 * frames + row + rows, :] = high
        for i, rel in enumerate(rels):
            high, low = split(grad_ref[:, rel * width : (rel + 1) * width])
            high, low = high.astype(F32), low.astype(F32)
            turned[i] = jnp.concatenate([high, high, low], axis=0).T.astype(BF16)

    x = x_all[from_ref[step]]
    for i in range(len(rels)):
        value = dot(turned[i], x, NN)
        for ref in added:
            value = value + ref[i]
        out_ref[i] = value


def weight_terms(sources, grad, own, other, rels, added=None):
    frames, features = grad.shape
    width = features // 4
    steps = sources.shape[0]
    whole = lambda array: pl.BlockSpec(array.shape, lambda s, src: (0,) * array.ndim)
    block = pl.BlockSpec((len(rels), width, width), lambda s, src: (0, 0, s))
    operands = [grad, *own, *other]
    in_specs = [whole(a) for a in operands]
    if added is not None:
        operands.append(added)
        in_specs.append(block)
    return call(
        partial(weight_body, len(own), spread_of(own, width), spread_of(other, width), rels),
        grid_spec=pltpu.PrefetchScalarGridSpec(
            num_scalar_prefetch=1,
            grid=(steps,),
            in_specs=in_specs,
            out_specs=block,
            scratch_shapes=[
                pltpu.VMEM((len(rels), width, 3 * frames), BF16),
                pltpu.VMEM((8, 3 * frames, width), BF16),
            ],
        ),
        out_shape=jax.ShapeDtypeStruct((len(rels), width, steps * width), F32),
        cost_estimate=cost(
            6 * frames * width * len(rels) * steps * width, 4 * width * len(rels) * steps * width
        ),
        name="weight_terms",
    )(sources, grad, *operands[1:])


def plane_gather(share):
    rows, depth = share.shape
    y, x = lax.axis_index("y"), lax.axis_index("x")
    first, second = share[:, : depth // 2], share[:, depth // 2 :]
    first = [first, lax.ppermute(first, "x", FLIP2)]
    second = [second, lax.ppermute(second, "y", FLIP2)]
    first += [lax.ppermute(piece, "y", FLIP2) for piece in first]
    second += [lax.ppermute(piece, "x", FLIP2) for piece in second]
    second = [second[0], second[2], second[1], second[3]]
    return first, second


def assemble_body(y_x_ref, *refs):
    first, second, out_ref = refs[:4], refs[4:8], refs[-1]
    rows, half = first[0].shape
    for rel in range(4):
        at = pl.multiple_of(
            (2 * (y_x_ref[0] ^ (rel // 2)) + (y_x_ref[1] ^ (rel % 2))) * rows, rows
        )
        out_ref[..., pl.ds(at, rows), :half] = first[rel][...].reshape(
            out_ref.shape[:-2] + (rows, half)
        )
        out_ref[..., pl.ds(at, rows), half:] = second[rel][...].reshape(
            out_ref.shape[:-2] + (rows, half)
        )


def assemble(y_x, first, second, layer=None, onto=None):
    rows, half = first[0].shape
    shape = (4 * rows, 2 * half)
    out_spec, aliases, extra, extra_specs = VMEM_SPEC, {}, [], []
    if layer is not None:
        out_spec = pl.BlockSpec((1, *shape), lambda i: (layer, 0, 0))
        if onto is not None:
            aliases, extra = {9: 0}, [onto]
            extra_specs = [pl.BlockSpec(memory_space=pl.ANY)]
        shape = (LAYERS, *shape)
    whole = pl.BlockSpec((rows, half), lambda i: (0, 0))
    return call(
        assemble_body,
        grid=(1,),
        out_shape=jax.ShapeDtypeStruct(shape, F32),
        in_specs=[SMEM_SPEC] + [whole] * 8 + extra_specs,
        out_specs=out_spec if layer is not None else pl.BlockSpec(shape, lambda i: (0, 0)),
        input_output_aliases=aliases,
        cost_estimate=cost(0, 8 * rows * half * 8),
        name="assemble",
    )(y_x, *first, *second, *extra)


def plane_scatter(total, first_axis, second_axis):
    dims = {"y": 1, "x": 2}

    def fold(array, axis, dim):
        at = lax.axis_index(axis)
        kept = lax.dynamic_index_in_dim(array, at, dim, keepdims=False)
        sent = lax.dynamic_index_in_dim(array, 1 - at, dim, keepdims=False)
        return kept + lax.ppermute(sent, axis, FLIP2)

    total = fold(total, first_axis, dims[first_axis])
    return fold(total, second_axis, 1)


def half_features(inputs, weights, gains, shifts, decays, biases, lengths, frame_mask, grad_out):
    width, slots = inputs.shape
    clips, frames = frame_mask.shape
    depth = weights.shape[2]
    blocks = 4 * width // LANES
    h, l, c = (lax.axis_index(name) for name in ("h", "l", "c"))
    b = 2 * lax.axis_index("y") + lax.axis_index("x")
    places, mine, theirs = [], [], []
    for rel in range(4):
        at_h, at_c = h ^ (rel // 2), c ^ (rel % 2)
        places.append(2 * at_h + at_c)
        mine.append((2 * at_h + l) * 2 + at_c)
        theirs.append((2 * at_h + (1 - l)) * 2 + at_c)
    place = jnp.stack(places).astype(jnp.int32)
    own_columns = jnp.stack(mine).astype(jnp.int32)
    other_columns = jnp.stack(theirs).astype(jnp.int32)
    sources = []
    for at_h in range(2):
        for at_l in range(2):
            for at_c in range(2):
                sources.append(4 * (l ^ at_l) + 2 * (h ^ at_h) + (c ^ at_c))
    sources = jnp.stack(sources).astype(jnp.int32)
    y_x = jnp.stack([lax.axis_index("y"), lax.axis_index("x")]).astype(jnp.int32)

    rows = width // 4
    near = swap(weights, 1)

    def far_of(share):
        first, second = plane_gather(lax.ppermute(share, "h", FLIP2))
        far = assemble(y_x, first, second)
        return [weights, near, far, swap(far, 1)]

    def share_of(layer):
        return lax.dynamic_slice(weights, (layer, b * rows, 0), (1, rows, depth))[0]

    clip = 2 * h + c
    seen = lax.dynamic_index_in_dim(frame_mask, clip, 0, keepdims=False)
    length = lax.dynamic_index_in_dim(lengths, clip, 0, keepdims=False)
    moments = jnp.arange(frames, dtype=jnp.int32)
    gate = ((moments < length) & ((seen == 1) | (moments == 0))).astype(F32)
    valid = jnp.broadcast_to(gate[:, None], (frames, LANES))

    params = jnp.stack([gains, shifts + biases, decays], axis=1).reshape(LAYERS, 3, width)
    params = lax.all_gather(params, ("h", "c"), axis=2, tiled=True)
    params = params.reshape(LAYERS, 3, blocks, LANES)

    def to_clips(array):
        pieces = pack(place, array, frames)
        return [swap(piece, rel) for rel, piece in enumerate(pieces)]

    def from_clips(pieces):
        return unpack(place, [swap(piece, rel) for rel, piece in enumerate(pieces)])

    def gather_sums(array):
        gathered = lax.all_gather(lax.all_gather(array, ("y", "x")), ("h", "c"))
        return gathered.reshape(16, *array.shape)

    own = to_clips(inputs)
    others = [swap_half(piece) for piece in own]
    half_weights = [far_of(share_of(0))]
    share, _ = lax.optimization_barrier((share_of(1), (own, others)))
    half_weights.append(far_of(share))
    upstream = None
    saved = []
    chunk_plan = (2, 1)
    for layer in range(LAYERS):
        other = others if layer == 0 else [swap_half(piece) for piece in own]
        z = project(own_columns, place, own, half_weights[layer], layer)[0]
        z, stats = project(other_columns, place, other, half_weights[layer], layer, z, valid)
        stats = gather_sums(stats)
        if layer == LAYERS - 1:
            turned, _ = lax.optimization_barrier((grad_out, stats))
            upstream = to_clips(turned)
        chunks = chunk_plan[layer]
        pieces = 4 if layer == LAYERS - 1 else 1
        state = jnp.zeros((blocks, LANES), F32)
        after, states, slopes = [], [], []
        for chunk in range(chunks):
            parts = own
            if own[0].shape[0] != frames:
                parts = [jnp.concatenate(own, axis=0)]
            *new, kept, slope, state = recur(
                chunk, chunks, place, gate, z, stats, params[layer], valid, state, parts, pieces
            )
            after.extend(new)
            states.append(kept)
            slopes.append(slope)
        saved.append((own, other, z, stats, states, slopes))
        own = after
    output = from_clips(own)

    ups = upstream
    results = [None] * LAYERS
    grad_weights = None
    for layer in range(LAYERS - 1, -1, -1):
        own, other, z, stats, states, slopes = saved[layer]
        weight = half_weights[layer]
        grad_pre, sums = back(place, gate, z, stats, params[layer], ups, states, slopes)
        sums = gather_sums(sums)
        grad_z, sent, sums = norm_back(
            other_columns, place, grad_pre, z, stats, params[layer], sums, valid, weight, layer
        )
        received = swap_half(sent)
        kept = own_terms(own_columns, grad_z, ups, weight, layer)
        ups = [kept, received]
        shares = []
        for half, axes in enumerate((("x", "y"), ("y", "x"))):
            some = sources[4 * half : 4 * half + 4]
            away = weight_terms(some, grad_z, own, other, (1, 3))
            total = weight_terms(some, grad_z, own, other, (0, 2), swap(away, 1))
            part = plane_scatter(total.reshape(2, 2, 2, rows, depth // 2), *axes)
            shares.append(part[0] + lax.ppermute(part[1], "h", FLIP2))
        grad_weights = assemble(
            y_x, *plane_gather(jnp.concatenate(shares, axis=1)), layer, grad_weights
        )
        sums = lax.dynamic_index_in_dim(
            sums.reshape(3, 4, width), 2 * h + c, axis=1, keepdims=False
        )
        results[layer] = sums
    grad_in = ups[0] + ups[1]
    grad_in = from_clips([grad_in[:, r * width : (r + 1) * width] for r in range(4)])
    sums = jnp.stack(results)
    return (output, grad_in, grad_weights, sums[:, 0], sums[:, 1], sums[:, 2], sums[:, 1])


def gelu_slope(value):
    return (
        0.5 * (1.0 + jax.scipy.special.erf(value / ROOT_TWO))
        + value * jnp.exp(-0.5 * value * value) / ROOT_TWO_PI
    )


def recur_step(decay, state, inputs):
    drive_t, valid_t = inputs
    pre = drive_t + decay * state
    state = state + valid_t * (jax.nn.gelu(pre, approximate=False) - state)
    return (state, state)


def back_step(decay, carry, inputs):
    upstream_t, valid_t, pre_t = inputs
    total = upstream_t + carry
    grad_pre = total * valid_t * gelu_slope(pre_t)
    carry = total * (1.0 - valid_t) + grad_pre * decay
    return (carry, grad_pre)


def add_piece(weight, piece):
    return jnp.dot(weight, piece, precision=HIGH, preferred_element_type=jnp.float32)


def weight_columns(grad_pre_norm, piece):
    return jnp.einsum("jf,kf->jk", grad_pre_norm, piece, precision=HIGH)


def split_features(inputs, weights, gains, shifts, decays, biases, lengths, frame_mask, grad_out):
    width, slots = inputs.shape
    clips, frames_len = frame_mask.shape
    frames = jnp.arange(frames_len, dtype=jnp.int32)
    valid_grid = (
        (frames[None, :] < lengths[:, None]) & ((frame_mask == 1) | (frames[None, :] == 0))
    ).astype(jnp.float32)
    valid = valid_grid.reshape(-1)
    valid_row = valid[None, :]
    valid_time = jnp.broadcast_to(valid_grid.T[:, :, None], (frames_len, clips, width)).reshape(
        frames_len, clips * width
    )
    count_local = jnp.sum(valid)

    def to_time(array):
        return jnp.transpose(array.reshape(width, clips, frames_len), (2, 1, 0)).reshape(
            frames_len, clips * width
        )

    def from_time(array):
        return jnp.transpose(array.reshape(frames_len, clips, width), (2, 1, 0)).reshape(
            width, slots
        )

    layer_in = inputs
    saved = []
    for layer_no in range(LAYERS):
        weight = weights[layer_no]
        gathered = lax.all_gather(layer_in, "neuron", axis=0, tiled=True)
        pre_norm = add_piece(weight, gathered)
        first_sum, count = lax.psum((jnp.sum(valid_row * pre_norm, axis=1), count_local), "batch")
        mean = first_sum / count
        centered = pre_norm - mean[:, None]
        var = lax.psum(jnp.sum(valid_row * centered * centered, axis=1), "batch") / count
        inv_std = lax.rsqrt(var + EPS)
        zhat = (pre_norm - mean[:, None]) * inv_std[:, None]
        drive = gains[layer_no][:, None] * zhat + (shifts[layer_no] + biases[layer_no])[:, None]
        drive_time = to_time(drive)
        decay_wide = jnp.tile(decays[layer_no], clips)
        start_state = jnp.zeros((clips * width,), jnp.float32)
        _, states = lax.scan(
            partial(recur_step, decay_wide), start_state, (drive_time, valid_time), unroll=8
        )
        saved.append((gathered, zhat, inv_std, drive_time, states, count))
        layer_in = layer_in + valid_row * from_time(states)
    upstream = grad_out
    grad_parts = [None] * LAYERS
    for layer_no in range(LAYERS - 1, -1, -1):
        gathered, zhat, inv_std, drive_time, states, count = saved[layer_no]
        decay_wide = jnp.tile(decays[layer_no], clips)
        gain = gains[layer_no]
        previous = jnp.concatenate([jnp.zeros_like(states[:1]), states[:-1]], axis=0)
        pre_time = drive_time + decay_wide[None, :] * previous
        grad_state = to_time(valid_row * upstream)
        start_carry = jnp.zeros((clips * width,), jnp.float32)
        _, grad_pre_time = lax.scan(
            partial(back_step, decay_wide),
            start_carry,
            (grad_state, valid_time, pre_time),
            reverse=True,
            unroll=8,
        )
        decay_local = jnp.sum(
            jnp.sum(grad_pre_time * previous, axis=0).reshape(clips, width), axis=0
        )
        grad_pre = from_time(grad_pre_time)
        gain_local = jnp.sum(grad_pre * zhat, axis=1)
        shift_local = jnp.sum(grad_pre, axis=1)
        grad_gain, grad_shift, grad_decay = lax.psum(
            (gain_local, shift_local, decay_local), "batch"
        )
        grad_pre_norm = (gain * inv_std)[:, None] * (
            grad_pre - valid_row * (grad_shift[:, None] + zhat * grad_gain[:, None]) / count
        )
        weight_local = weight_columns(grad_pre_norm, gathered)
        input_terms = jnp.einsum("jk,jf->kf", weights[layer_no], grad_pre_norm, precision=HIGH)
        input_grad = lax.psum_scatter(input_terms, "neuron", scatter_dimension=0, tiled=True)
        grad_weight = lax.psum(weight_local, "batch")
        upstream = upstream + input_grad
        grad_parts[layer_no] = (grad_weight, grad_gain, grad_shift, grad_decay)
    grad_weights = jnp.stack([grad_parts[layer_no][0] for layer_no in range(LAYERS)])
    grad_gains = jnp.stack([grad_parts[layer_no][1] for layer_no in range(LAYERS)])
    grad_shifts = jnp.stack([grad_parts[layer_no][2] for layer_no in range(LAYERS)])
    grad_decays = jnp.stack([grad_parts[layer_no][3] for layer_no in range(LAYERS)])
    return (layer_in, upstream, grad_weights, grad_gains, grad_shifts, grad_decays, grad_shifts)


def solution(mesh):
    if (mesh.shape["batch"], mesh.shape["neuron"]) == (4, 8):
        cut = Mesh(mesh.devices.reshape(2, 2, 2, 2, 2), ("y", "x", "h", "l", "c"))
        batch, neuron, body = ("y", "x"), ("h", "l", "c"), half_features
    else:
        cut, batch, neuron, body = mesh, "batch", "neuron", split_features
    in_specs = (
        P(neuron, batch),
        P(None, neuron, None),
        P(None, neuron),
        P(None, neuron),
        P(None, neuron),
        P(None, neuron),
        P(batch),
        P(batch, None),
        P(neuron, batch),
    )
    out_specs = (
        P(neuron, batch),
        P(neuron, batch),
        P(None, neuron, None),
        P(None, neuron),
        P(None, neuron),
        P(None, neuron),
        P(None, neuron),
    )
    return jax.shard_map(
        body, mesh=cut, in_specs=in_specs, out_specs=out_specs, check_vma=False
    )
```

```python
from functools import partial
import math

import jax
import jax.numpy as jnp
from jax import lax
from jax.experimental import pallas as pl
from jax.experimental.pallas import tpu as pltpu
from jax.sharding import Mesh, PartitionSpec as P

LAYERS = 2
EPS = 1e-05
HIGH = lax.Precision.HIGHEST
ROOT_TWO = math.sqrt(2.0)
ROOT_TWO_PI = math.sqrt(2.0 * math.pi)
F32 = jnp.float32
BF16 = jnp.bfloat16
LANES = 128
VMEM_LIMIT = 48 * 1024 * 1024
SMEM_SPEC = pl.BlockSpec(memory_space=pltpu.SMEM)
VMEM_SPEC = pl.BlockSpec(memory_space=pltpu.VMEM)


FLIP2 = [(0, 1), (1, 0)]


def flip_of(rel):
    if rel == 1:
        return "c", FLIP2
    if rel == 2:
        return "h", FLIP2
    return ("h", "c"), [(i, i ^ 3) for i in range(4)]


def swap(array, rel):
    if rel == 0:
        return array
    axes, pairs = flip_of(rel)
    return lax.ppermute(array, axes, pairs)


def swap_half(array):
    return lax.ppermute(array, "l", FLIP2)


def split(value):
    high = value.astype(BF16)
    return high, (value - high.astype(F32)).astype(BF16)


def dot(a, b, dims):
    return lax.dot_general(a, b, (dims, ((), ())), preferred_element_type=F32)


NT = ((1,), (1,))
NN = ((1,), (0,))


def call(body, **kwargs):
    return pl.pallas_call(
        body,
        compiler_params=pltpu.CompilerParams(vmem_limit_bytes=VMEM_LIMIT),
        **kwargs,
    )


def cost(flops, byte_count):
    return pl.CostEstimate(flops=int(flops) // 64, bytes_accessed=int(byte_count) // 64, transcendentals=0)


def pack_body(frames, place_ref, in_ref, *refs):
    outs, turned = refs[:4], refs[4]
    slots = in_ref.shape[1]
    for start in range(0, slots, LANES):
        turned[start : start + LANES, :] = in_ref[:, start : start + LANES].T
    for rel in range(4):
        first = pl.multiple_of(place_ref[rel] * frames, 8)
        outs[rel][...] = turned[pl.ds(first, frames), :]


def pack(place, array, frames):
    width, slots = array.shape
    return call(
        partial(pack_body, frames),
        out_shape=[jax.ShapeDtypeStruct((frames, width), F32)] * 4,
        in_specs=[SMEM_SPEC, VMEM_SPEC],
        out_specs=[VMEM_SPEC] * 4,
        scratch_shapes=[pltpu.VMEM((slots, width), F32)],
        cost_estimate=cost(0, 8 * width * slots),
        name="pack",
    )(place, array)


def unpack_body(frames, place_ref, *refs):
    ins, out_ref, turned = refs[:4], refs[4], refs[5]
    slots = out_ref.shape[1]
    for rel in range(4):
        first = pl.multiple_of(place_ref[rel] * frames, 8)
        turned[pl.ds(first, frames), :] = ins[rel][...]
    for start in range(0, slots, LANES):
        out_ref[:, start : start + LANES] = turned[start : start + LANES, :].T


def unpack(place, pieces):
    frames, width = pieces[0].shape
    slots = 4 * frames
    return call(
        partial(unpack_body, frames),
        out_shape=jax.ShapeDtypeStruct((width, slots), F32),
        in_specs=[SMEM_SPEC] + [VMEM_SPEC] * 4,
        out_specs=VMEM_SPEC,
        scratch_shapes=[pltpu.VMEM((slots, width), F32)],
        cost_estimate=cost(0, 8 * width * slots),
        name="unpack",
    )(place, *pieces)


def spread_of(parts, width):
    spots, row, column = [], 0, 0
    for part in parts:
        spots.append((row, column))
        if part.shape[1] == width:
            column += width
        else:
            row += part.shape[0]
    return spots


def put_pairs(place_ref, spots, parts, high_ref, low_ref):
    width = high_ref.shape[2] // 2
    for (row, column), part in zip(spots, parts):
        rows, columns = part.shape
        for start in range(0, columns, width):
            rel = (column + start) // width
            at = pl.multiple_of((place_ref[rel] & 1) * width, width)
            high, low = split(part[:, start : start + width])
            high_ref[rel // 2, row : row + rows, pl.ds(at, width)] = high
            low_ref[rel // 2, row : row + rows, pl.ds(at, width)] = low


def project_body(n_parts, spots, with_acc, with_stats, flat, cols_ref, place_ref, *refs):
    del cols_ref
    parts, refs = refs[:n_parts], refs[n_parts:]
    weights, refs = refs[:4], refs[4:]
    if with_acc:
        acc_ref, refs = refs[0], refs[1:]
    if with_stats:
        valid_ref, refs = refs[0], refs[1:]
    out_ref, refs = refs[0], refs[1:]
    if with_stats:
        stats_ref, refs = refs[0], refs[1:]
    if flat:
        flat_ref, refs = refs[0], refs[1:]
    x_high, x_low = refs
    step = pl.program_id(0)
    width = x_high.shape[2] // 2

    @pl.when(step == 0)
    def _():
        put_pairs(place_ref, spots, parts, x_high, x_low)
        if flat:
            for (row, column), part in zip(spots, parts):
                rows, columns = part.shape
                flat_ref[row : row + rows, column : column + columns] = part[...]

    high, low = x_high[step], x_low[step]
    stacked = jnp.concatenate([high, low, high], axis=1)
    for block in range(4):
        w_high, w_low = split(weights[block][...].reshape(width, 2 * width))
        columns = slice(block * width, (block + 1) * width)
        value = dot(stacked, jnp.concatenate([w_high, w_high, w_low], axis=1), NT)

        @pl.when(step == 0)
        def _():
            out_ref[:, columns] = value + acc_ref[:, columns] if with_acc else value

        @pl.when(step == 1)
        def _():
            total = out_ref[:, columns] + value
            out_ref[:, columns] = total
            if with_stats:
                valid = valid_ref[...]
                own = jnp.sum(valid, axis=0, keepdims=True)
                per = width // LANES
                for row in range(per):
                    z = total[:, row * LANES : (row + 1) * LANES]
                    sums = jnp.sum(valid * z, axis=0, keepdims=True)
                    centred = valid * (z - sums / own)
                    squares = jnp.sum(centred * centred, axis=0, keepdims=True)
                    at = place_ref[block] * per + row
                    stats_ref[0, pl.ds(at, 1), :] = sums
                    stats_ref[1, pl.ds(at, 1), :] = squares
                    stats_ref[2, pl.ds(at, 1), :] = own


def weight_specs(weights, layer):
    specs = []
    for weight in weights:
        width = weight.shape[-2]
        if weight.ndim == 3:
            specs.append(
                pl.BlockSpec((1, width, 2 * width), lambda s, cols, *_: (layer, 0, cols[s]))
            )
        else:
            specs.append(pl.BlockSpec((width, 2 * width), lambda s, cols, *_: (0, cols[s])))
    return specs


def project(columns, place, parts, weights, layer, acc=None, valid=None, flat=False):
    width = weights[0].shape[-2]
    frames = sum(p.shape[0] for p in parts if p.shape[1] != width) or parts[0].shape[0]
    full = pl.BlockSpec(memory_space=pltpu.VMEM)
    in_specs = [full] * len(parts)
    in_specs += weight_specs(weights, layer)
    operands = list(parts) + list(weights)
    array = jax.ShapeDtypeStruct((frames, 4 * width), F32)
    array_spec = pl.BlockSpec((frames, 4 * width), lambda s, cols, place: (0, 0))
    out_shape, out_specs = [array], [array_spec]
    if acc is not None:
        in_specs.append(full)
        operands.append(acc)
    if valid is not None:
        in_specs.append(full)
        operands.append(valid)
        rows = 4 * width // LANES
        out_shape.append(jax.ShapeDtypeStruct((3, rows, LANES), F32))
        out_specs.append(pl.BlockSpec((3, rows, LANES), lambda s, cols, place: (0, 0, 0)))
    if flat:
        out_shape.append(array)
        out_specs.append(array_spec)
    return call(
        partial(
            project_body,
            len(parts),
            spread_of(parts, width),
            acc is not None,
            valid is not None,
            flat,
        ),
        grid_spec=pltpu.PrefetchScalarGridSpec(
            num_scalar_prefetch=2,
            grid=(2,),
            in_specs=in_specs,
            out_specs=out_specs,
            scratch_shapes=[pltpu.VMEM((2, frames, 2 * width), BF16)] * 2,
        ),
        out_shape=out_shape,
        cost_estimate=cost(2 * 3 * frames * 16 * width * width, 4 * 16 * width * width),
        name="project",
    )(columns, place, *operands)


def to_relative(place_ref, spread, rows_ref, value, slot):
    per = value.shape[0] // 4
    spread[...] = value
    for rel in range(4):
        first = place_ref[rel] * per
        for row in range(per):
            rows_ref[slot, rel * per + row : rel * per + row + 1, :] = spread[
                pl.ds(first + row, 1), :
            ]


def norm_terms(stats_ref):
    devices = stats_ref.shape[0]
    count = stats_ref[0, 2]
    total = stats_ref[0, 0]
    for i in range(1, devices):
        count = count + stats_ref[i, 2]
        total = total + stats_ref[i, 0]
    mean = total / count
    squares = jnp.zeros_like(mean)
    for i in range(devices):
        away = stats_ref[i, 0] / stats_ref[i, 2] - mean
        squares = squares + (stats_ref[i, 1] + stats_ref[i, 2] * away * away)
    return count, mean, lax.rsqrt(squares / count + EPS)


def recur_body(n_parts, spots, out_cols, first, width, place_ref, gate_ref, z_ref, stats_ref, params_ref, valid_ref, start_ref, *refs):
    parts, refs = refs[:n_parts], refs[n_parts:]
    n_out = len(out_cols)
    outs, refs = refs[:n_out], refs[n_out:]
    state_ref, slope_ref, last_ref, rows, spread, drive_s, state_s, slope_s = refs
    frames = z_ref.shape[0]
    blocks = z_ref.shape[1] // LANES
    _, mean, inv_std = norm_terms(stats_ref)
    to_relative(place_ref, spread, rows, mean, 0)
    to_relative(place_ref, spread, rows, params_ref[0] * inv_std, 1)
    to_relative(place_ref, spread, rows, params_ref[1], 2)
    to_relative(place_ref, spread, rows, params_ref[2], 3)
    for row in range(blocks):
        z = z_ref[:, row * LANES : (row + 1) * LANES]
        drive_s[row * frames : (row + 1) * frames, :] = (
            z - rows[0, row : row + 1, :]
        ) * rows[1, row : row + 1, :] + rows[2, row : row + 1, :]
    decay = rows[3]

    def step(t, state):
        at = pl.ds(t, blocks, stride=frames)
        pre = drive_s[at, :] + decay * state
        half = 0.5 + 0.5 * lax.erf(pre * (1.0 / ROOT_TWO))
        gate = gate_ref[first + t] > 0.0
        slope = half + pre * jnp.exp(-0.5 * pre * pre) * (1.0 / ROOT_TWO_PI)
        state = jnp.where(gate, pre * half, state)
        state_s[at, :] = state
        slope_s[at, :] = jnp.where(gate, slope, 0.0)
        return state

    last_ref[...] = lax.fori_loop(0, frames, step, start_ref[...], unroll=8)
    valid = valid_ref[...]
    for row in range(blocks):
        lanes = slice(row * LANES, (row + 1) * LANES)
        state = state_s[row * frames : (row + 1) * frames, :]
        state_ref[:, lanes] = state
        slope_ref[:, lanes] = slope_s[row * frames : (row + 1) * frames, :]
        for (_, column), part in zip(spots, parts):
            if column <= row * LANES < column + part.shape[1]:
                x = part[:, row * LANES - column : (row + 1) * LANES - column]
        for column, out in zip(out_cols, outs):
            if column <= row * LANES < column + out.shape[1]:
                out[:, row * LANES - column : (row + 1) * LANES - column] = x + valid * state


def recur(chunk, chunks, place, gate, z, stats, params, valid, start, parts, pieces):
    frames = z.shape[0] // chunks
    features = z.shape[1]
    width = features // 4
    blocks = features // LANES
    row_block = lambda columns: pl.BlockSpec((frames, columns), lambda i: (chunk, 0))
    whole = lambda array: pl.BlockSpec(array.shape, lambda i: (0,) * array.ndim)
    part_specs = [row_block(p.shape[1]) if p.shape[0] == z.shape[0] else whole(p) for p in parts]
    n_out = pieces
    out_width = features // n_out
    tile = jax.ShapeDtypeStruct((blocks, LANES), F32)
    full = jax.ShapeDtypeStruct((frames, features), F32)
    out_shape = [jax.ShapeDtypeStruct((frames, out_width), F32)] * n_out + [full, full, tile]
    return call(
        partial(
            recur_body,
            len(parts),
            spread_of(parts, width),
            [i * out_width for i in range(n_out)],
            chunk * frames,
            width,
        ),
        grid=(1,),
        in_specs=[
            SMEM_SPEC,
            SMEM_SPEC,
            row_block(features),
            whole(stats),
            whole(params),
            row_block(LANES),
            whole(start),
        ]
        + part_specs,
        out_specs=[whole(s) for s in out_shape],
        out_shape=out_shape,
        scratch_shapes=[
            pltpu.VMEM((4, blocks, LANES), F32),
            pltpu.VMEM((blocks, LANES), F32),
        ]
        + [pltpu.VMEM((blocks * frames, LANES), F32)] * 3,
        cost_estimate=cost(100 * frames * features, 20 * frames * features),
        name="recur",
    )(place, gate, z, stats, params, valid, start, *parts)


def back_body(n_parts, spots, n_state, place_ref, gate_ref, z_ref, stats_ref, params_ref, *refs):
    parts, refs = refs[:n_parts], refs[n_parts:]
    states, refs = refs[:n_state], refs[n_state:]
    slopes, refs = refs[:n_state], refs[n_state:]
    grad_ref, sums_ref, rows, spread, up_s, state_s, slope_s = refs
    frames = z_ref.shape[0]
    blocks = z_ref.shape[1] // LANES
    tall = frames + 8
    _, mean, inv_std = norm_terms(stats_ref)
    to_relative(place_ref, spread, rows, mean, 0)
    to_relative(place_ref, spread, rows, inv_std, 1)
    to_relative(place_ref, spread, rows, params_ref[2], 2)
    for row in range(blocks):
        lanes = slice(row * LANES, (row + 1) * LANES)
        base = row * frames
        up = None
        for (top, column), part in zip(spots, parts):
            if column <= row * LANES < column + part.shape[1] and part.shape[0] == frames:
                value = part[:, row * LANES - column : (row + 1) * LANES - column]
                up = value if up is None else up + value
        up_s[base : base + frames, :] = up
        state_s[row * tall : row * tall + 8, :] = jnp.zeros((8, LANES), F32)
        first = 0
        for state, slope in zip(states, slopes):
            some = state.shape[0]
            at = row * tall + 8 + first
            state_s[at : at + some, :] = state[:, lanes]
            slope_s[base + first : base + first + some, :] = slope[:, lanes]
            first += some
    decay = rows[2]

    def step(i, carry):
        t = frames - 1 - i
        at = pl.ds(t, blocks, stride=frames)
        slope = slope_s[at, :]
        gate = gate_ref[t]
        total = gate * up_s[at, :] + carry
        up_s[at, :] = total * slope
        return total * (slope * decay + (1.0 - gate))

    lax.fori_loop(0, frames, step, jnp.zeros((blocks, LANES), F32), unroll=8)
    per = blocks // 4
    for row in range(blocks):
        lanes = slice(row * LANES, (row + 1) * LANES)
        base = row * frames
        grad = up_s[base : base + frames, :]
        grad_ref[:, lanes] = grad
        zhat = (z_ref[:, lanes] - rows[0, row : row + 1, :]) * rows[1, row : row + 1, :]
        before = state_s[row * tall + 7 : row * tall + 7 + frames, :]
        at = place_ref[row // per] * per + row % per
        for slot, value in enumerate((grad * zhat, grad, grad * before)):
            sums_ref[slot, pl.ds(at, 1), :] = jnp.sum(value, axis=0, keepdims=True)


def spots_of_sum(parts, width):
    spots, column = [], 0
    for part in parts:
        if part.shape[1] == width:
            spots.append((0, column))
            column += width
        else:
            spots.append((0, 0))
    return spots


def back(place, gate, z, stats, params, ups, states, slopes):
    frames, features = z.shape
    width = features // 4
    blocks = features // LANES
    return call(
        partial(back_body, len(ups), spots_of_sum(ups, width), len(states)),
        in_specs=[SMEM_SPEC] * 2 + [VMEM_SPEC] * (3 + len(ups) + 2 * len(states)),
        out_specs=[VMEM_SPEC] * 2,
        out_shape=[
            jax.ShapeDtypeStruct((frames, features), F32),
            jax.ShapeDtypeStruct((3, blocks, LANES), F32),
        ],
        scratch_shapes=[
            pltpu.VMEM((3, blocks, LANES), F32),
            pltpu.VMEM((blocks, LANES), F32),
            pltpu.VMEM((blocks * frames, LANES), F32),
            pltpu.VMEM((blocks * (frames + 8), LANES), F32),
            pltpu.VMEM((blocks * frames, LANES), F32),
        ],
        cost_estimate=cost(30 * frames * features, 20 * frames * features),
        name="back",
    )(place, gate, z, stats, params, *ups, *states, *slopes)


def input_terms(place_ref, high_s, low_s, weights, step):
    width = high_s.shape[2]
    left, right = [], []
    for block, weight in enumerate(weights):
        w_high, w_low = split(weight[...].reshape(width, 2 * width))
        left += [high_s[block], low_s[block], high_s[block]]
        right += [w_high, w_high, w_low]
    return dot(jnp.concatenate(left, axis=1), jnp.concatenate(right, axis=0), NN)


def norm_back_body(cols_ref, place_ref, grad_ref, z_ref, stats_ref, params_ref, sums_ref, valid_ref, w0, w1, w2, w3, out_ref, term_ref, sums_out_ref, rows, spread, high_s, low_s):
    del cols_ref
    blocks = z_ref.shape[1] // LANES
    width = high_s.shape[2]
    per = width // LANES

    @pl.when(pl.program_id(0) == 0)
    def _():
        count, mean, inv_std = norm_terms(stats_ref)
        to_relative(place_ref, spread, rows, mean, 0)
        to_relative(place_ref, spread, rows, inv_std, 1)
        to_relative(place_ref, spread, rows, params_ref[0] * inv_std, 2)
        sums = sums_ref[0]
        for i in range(1, sums_ref.shape[0]):
            sums = sums + sums_ref[i]
        sums_out_ref[...] = sums
        to_relative(place_ref, spread, rows, sums[0] / count, 3)
        to_relative(place_ref, spread, rows, sums[1] / count, 4)
        valid = valid_ref[...]
        for row in range(blocks):
            lanes = slice(row * LANES, (row + 1) * LANES)
            one = lambda slot: rows[slot, row : row + 1, :]
            zhat = (z_ref[:, lanes] - one(0)) * one(1)
            value = one(2) * (grad_ref[:, lanes] - valid * (one(4) + zhat * one(3)))
            out_ref[:, lanes] = value
            high, low = split(value)
            inner = slice((row % per) * LANES, (row % per + 1) * LANES)
            high_s[row // per, :, inner] = high
            low_s[row // per, :, inner] = low

    value = input_terms(place_ref, high_s, low_s, (w0, w1, w2, w3), pl.program_id(0))
    for pair in range(2):
        at = pl.multiple_of(((place_ref[0] & 1) ^ pair) * width, width)
        term_ref[:, pl.ds(at, width)] = value[:, pair * width : (pair + 1) * width]


def norm_back(columns, place, grad, z, stats, params, sums, valid, weights, layer):
    frames, features = z.shape
    width = features // 4
    blocks = features // LANES
    whole = lambda array: pl.BlockSpec(array.shape, lambda s, cols, place: (0,) * array.ndim)
    operands = [grad, z, stats, params, sums, valid]
    full = jax.ShapeDtypeStruct((frames, features), F32)
    return call(
        norm_back_body,
        grid_spec=pltpu.PrefetchScalarGridSpec(
            num_scalar_prefetch=2,
            grid=(2,),
            in_specs=[whole(a) for a in operands] + weight_specs(weights, layer),
            out_specs=[
                whole(full),
                pl.BlockSpec((frames, 2 * width), lambda s, cols, place: (0, s)),
                pl.BlockSpec((3, blocks, LANES), lambda s, cols, place: (0, 0, 0)),
            ],
            scratch_shapes=[
                pltpu.VMEM((5, blocks, LANES), F32),
                pltpu.VMEM((blocks, LANES), F32),
                pltpu.VMEM((4, frames, width), BF16),
                pltpu.VMEM((4, frames, width), BF16),
            ],
        ),
        out_shape=[full, full, jax.ShapeDtypeStruct((3, blocks, LANES), F32)],
        cost_estimate=cost(6 * frames * features * features, 4 * features * features),
        name="norm_back",
    )(columns, place, *operands, *weights)


def own_terms_body(n_ups, piecewise, cols_ref, place_ref, grad_ref, *refs):
    del cols_ref
    ups, refs = refs[:n_ups], refs[n_ups:]
    weights, refs = refs[:4], refs[4:]
    out_ref, high_s, low_s = refs
    width = high_s.shape[2]
    step = pl.program_id(0)

    @pl.when(step == 0)
    def _():
        for block in range(4):
            high, low = split(grad_ref[:, block * width : (block + 1) * width])
            high_s[block] = high
            low_s[block] = low

    value = input_terms(place_ref, high_s, low_s, weights, step)
    for pair in range(2):
        at = pl.multiple_of(((place_ref[0] & 1) ^ pair) * width, width)
        out_ref[:, pl.ds(at, width)] = value[:, pair * width : (pair + 1) * width]
    if piecewise:
        for block in range(4):

            @pl.when(step == block // 2)
            def _():
                lanes = slice((block % 2) * width, (block % 2 + 1) * width)
                out_ref[:, lanes] += ups[block][...]
    else:
        for up in ups:
            out_ref[...] += up[...]


def own_terms(columns, place, grad, ups, weights, layer):
    frames, features = grad.shape
    width = features // 4
    piecewise = ups[0].shape[1] == width
    whole = lambda array: pl.BlockSpec(array.shape, lambda s, cols, place: (0,) * array.ndim)
    step_block = pl.BlockSpec((frames, 2 * width), lambda s, cols, place: (0, s))
    return call(
        partial(own_terms_body, len(ups), piecewise),
        grid_spec=pltpu.PrefetchScalarGridSpec(
            num_scalar_prefetch=2,
            grid=(2,),
            in_specs=[whole(grad)]
            + [whole(u) if piecewise else step_block for u in ups]
            + weight_specs(weights, layer),
            out_specs=step_block,
            scratch_shapes=[pltpu.VMEM((4, frames, width), BF16)] * 2,
        ),
        out_shape=jax.ShapeDtypeStruct((frames, features), F32),
        cost_estimate=cost(6 * frames * features * features, 4 * features * features),
        name="own_terms",
    )(columns, place, grad, *ups, *weights)


def weight_body(n_chunks, lists_ref, place_ref, grad_ref, near_ref, *refs):
    del lists_ref
    per_group = []
    for _ in range(4):
        per_group.append(refs[:n_chunks])
        refs = refs[n_chunks:]
    kept_first, sent_first, kept_second, sent_second, turned, ordered, x_all = refs
    step = pl.program_id(0)
    width = x_all.shape[1]
    frames = grad_ref.shape[0]
    padded = x_all.shape[0] // 6
    rows = width // 4

    @pl.when(step == 0)
    def _():
        turned[...] = jnp.zeros_like(turned)
        x_all[...] = jnp.zeros_like(x_all)
        for clip in range(2):
            for dh in range(2):
                if clip == 0:
                    part = grad_ref[:, 2 * dh * width : (2 * dh + 1) * width]
                else:
                    part = near_ref[:, dh * width : (dh + 1) * width]
                high, low = split(part.T)
                for slot, value in enumerate((high, high, low)):
                    first = (3 * clip + slot) * padded
                    turned[dh * width : (dh + 1) * width, first : first + frames] = value
        for half in range(2):
            for i in range(4):
                for dh in range(2):
                    dy, dx = (i % 2, i // 2) if half == 0 else (i // 2, i % 2)
                    y, x = place_ref[4] ^ dy, place_ref[5] ^ dx
                    at = pl.multiple_of(dh * width + (2 * y + x) * rows, rows)
                    to = (2 * i + dh) * rows
                    ordered[half, to : to + rows, :] = turned[pl.ds(at, rows), :]

    for half in range(2):

        @pl.when(lax.rem(step, 4) // 2 == half)
        def _():
            for clip in range(2):
                row = 0
                for part in per_group[2 * clip + half]:
                    some = part.shape[0]
                    high, low = split(part[...])
                    for slot, value in enumerate((high, low, high)):
                        first = (3 * clip + slot) * padded + row
                        x_all[first : first + some, :] = value
                    row += some

    for half, (kept, sent) in enumerate(((kept_first, sent_first), (kept_second, sent_second))):

        @pl.when(step // 4 == half)
        def _():
            value = dot(ordered[half], x_all[...], NN)
            kept[...] = value[: 2 * width // 2].reshape(kept.shape)
            sent[...] = value[2 * width // 2 :].reshape(sent.shape)


def weight_terms(lists, place, grad, near, groups):
    frames, features = grad.shape
    width = features // 4
    padded = -(-frames // LANES) * LANES
    whole = lambda array: pl.BlockSpec(array.shape, lambda s, src, place: (0,) * array.ndim)
    operands, in_specs = [grad, near], [whole(grad), whole(near)]
    for i, group in enumerate(groups):
        for part in group:
            operands.append(part)
            at = 8 * (i // 2)
            in_specs.append(
                pl.BlockSpec(
                    (part.shape[0], width), lambda s, src, place, at=at: (0, src[at + s])
                )
            )
    shape = (2, 2, width // 4, 4 * width)
    first = pl.BlockSpec(
        shape[:3] + (width,), lambda s, src, place: (0, 0, 0, src[16 + jnp.minimum(s, 3)])
    )
    second = pl.BlockSpec(
        shape[:3] + (width,), lambda s, src, place: (0, 0, 0, src[16 + jnp.maximum(s, 4)])
    )
    return call(
        partial(weight_body, len(groups[0])),
        grid_spec=pltpu.PrefetchScalarGridSpec(
            num_scalar_prefetch=2,
            grid=(8,),
            in_specs=in_specs,
            out_specs=[first, first, second, second],
            scratch_shapes=[
                pltpu.VMEM((2 * width, 6 * padded), BF16),
                pltpu.VMEM((2, 2 * width, 6 * padded), BF16),
                pltpu.VMEM((6 * padded, width), BF16),
            ],
        ),
        out_shape=[jax.ShapeDtypeStruct(shape, F32)] * 4,
        cost_estimate=cost(12 * frames * 2 * width * 8 * width, 4 * 16 * width * width),
        name="weight_terms",
    )(lists, place, *operands)


def plane_gather(first, second=None):
    if second is None:
        half = first.shape[1] // 2
        first, second = first[:, :half], first[:, half:]
    first = [first, lax.ppermute(first, "x", FLIP2)]
    second = [second, lax.ppermute(second, "y", FLIP2)]
    first += [lax.ppermute(piece, "y", FLIP2) for piece in first]
    second += [lax.ppermute(piece, "x", FLIP2) for piece in second]
    second = [second[0], second[2], second[1], second[3]]
    return first, second


def assemble_body(y_x_ref, *refs):
    first, second, out_ref = refs[:4], refs[4:8], refs[-1]
    rows, half = first[0].shape
    for rel in range(4):
        at = pl.multiple_of(
            (2 * (y_x_ref[0] ^ (rel // 2)) + (y_x_ref[1] ^ (rel % 2))) * rows, rows
        )
        out_ref[..., pl.ds(at, rows), :half] = first[rel][...].reshape(
            out_ref.shape[:-2] + (rows, half)
        )
        out_ref[..., pl.ds(at, rows), half:] = second[rel][...].reshape(
            out_ref.shape[:-2] + (rows, half)
        )


def assemble(y_x, first, second, layer=None, onto=None):
    rows, half = first[0].shape
    shape = (4 * rows, 2 * half)
    out_spec, aliases, extra, extra_specs = VMEM_SPEC, {}, [], []
    if layer is not None:
        out_spec = pl.BlockSpec((1, *shape), lambda i: (layer, 0, 0))
        if onto is not None:
            aliases, extra = {9: 0}, [onto]
            extra_specs = [pl.BlockSpec(memory_space=pl.ANY)]
        shape = (LAYERS, *shape)
    whole = pl.BlockSpec((rows, half), lambda i: (0, 0))
    return call(
        assemble_body,
        grid=(1,),
        out_shape=jax.ShapeDtypeStruct(shape, F32),
        in_specs=[SMEM_SPEC] + [whole] * 8 + extra_specs,
        out_specs=out_spec if layer is not None else pl.BlockSpec(shape, lambda i: (0, 0)),
        input_output_aliases=aliases,
        cost_estimate=cost(0, 8 * rows * half * 8),
        name="assemble",
    )(y_x, *first, *second, *extra)


def after(value, *others):
    return lax.optimization_barrier((value, others))[0]


def half_features(inputs, weights, gains, shifts, decays, biases, lengths, frame_mask, grad_out):
    width, slots = inputs.shape
    clips, frames = frame_mask.shape
    depth = weights.shape[2]
    blocks = 4 * width // LANES
    y, x, h, l, c = (lax.axis_index(name) for name in ("y", "x", "h", "l", "c"))
    b = 2 * y + x
    numbers = [2 * (h ^ (rel // 2)) + (c ^ (rel % 2)) for rel in range(4)] + [y, x]
    place = jnp.stack(numbers).astype(jnp.int32)
    own_columns = jnp.stack([2 * h + l, 2 * (1 - h) + l]).astype(jnp.int32)
    other_columns = jnp.stack([2 * h + 1 - l, 2 * (1 - h) + 1 - l]).astype(jnp.int32)
    mine, theirs, spots = [], [], []
    for at_h in range(2):
        for dl in range(2):
            for dc in range(2):
                mine.append(2 * (h ^ at_h) + dc)
                theirs.append(2 * (h ^ at_h) + (1 - dc))
                spots.append(2 * (l ^ dl) + (c ^ dc))
    lists = jnp.stack(mine + theirs + spots).astype(jnp.int32)
    y_x = place[4:]
    rows = width // 4

    clip = 2 * h + c
    seen = lax.dynamic_index_in_dim(frame_mask, clip, 0, keepdims=False)
    length = lax.dynamic_index_in_dim(lengths, clip, 0, keepdims=False)
    moments = jnp.arange(frames, dtype=jnp.int32)
    gate = ((moments < length) & ((seen == 1) | (moments == 0))).astype(F32)
    valid = jnp.broadcast_to(gate[:, None], (frames, LANES))

    params = jnp.stack([gains, shifts + biases, decays], axis=1).reshape(LAYERS, 3, width)
    params = lax.all_gather(params, ("h", "c"), axis=2, tiled=True)
    params = params.reshape(LAYERS, 3, blocks, LANES)

    def gather_sums(array):
        gathered = lax.all_gather(lax.all_gather(array, ("y", "x")), ("h", "c"))
        return gathered.reshape(16, *array.shape)

    def far_share(layer, *before):
        share = lax.dynamic_slice(weights, (layer, b * rows, 0), (1, rows, depth))[0]
        return lax.ppermute(after(share, *before), "h", FLIP2)

    def half_of(share):
        far = assemble(y_x, *plane_gather(share))
        return [weights, near, far, swap(far, 1)]

    near = swap(weights, 1)
    share = far_share(0)
    pieces = pack(place, inputs, frames)
    own = [pieces[0], swap(pieces[1], 1)]
    others = [swap_half(piece) for piece in own]
    far_pieces = after(pieces[2:], share)
    own += [swap(piece, 2 + i) for i, piece in enumerate(far_pieces)]
    others += [swap_half(piece) for piece in own[2:]]
    half_weights = [half_of(share)]
    share = far_share(1, own)

    upstream = None
    saved = []
    chunk_plan = (2, 1)
    for layer in range(LAYERS):
        other = others if layer == 0 else [swap_half(piece) for piece in own]
        flat = layer == 0
        z, *own_flat = project(
            own_columns, place, own, half_weights[layer], layer, flat=flat
        )
        if layer == LAYERS - 1:
            turned = pack(place, after(grad_out, z), frames)
            upstream = [swap(piece, rel) for rel, piece in enumerate(turned)]
        z, stats, *other_flat = project(
            other_columns, place, other, half_weights[layer], layer, z, valid, flat=flat
        )
        if layer == 0:
            half_weights.append(half_of(after(share, z)))
        stats = gather_sums(stats)
        chunks = chunk_plan[layer]
        pieces = 4 if layer == LAYERS - 1 else 1
        state = jnp.zeros((blocks, LANES), F32)
        following, states, slopes = [], [], []
        for chunk in range(chunks):
            parts = own
            if own[0].shape[0] != frames:
                parts = [jnp.concatenate(own, axis=0)]
            *new, kept, slope, state = recur(
                chunk, chunks, place, gate, z, stats, params[layer], valid, state, parts, pieces
            )
            following.extend(new)
            states.append(kept)
            slopes.append(slope)
        groups = [own_flat, other_flat] if flat else [own, other]
        groups = groups + [[swap(after(p, z), 1) for p in group] for group in groups]
        saved.append((groups, z, stats, states, slopes))
        own = following
    output = [swap(piece, rel) for rel, piece in enumerate(own)]

    ups = upstream
    results = [None] * LAYERS
    grad_weights = None
    for layer in range(LAYERS - 1, -1, -1):
        groups, z, stats, states, slopes = saved[layer]
        weight = half_weights[layer]
        grad_pre, sums = back(place, gate, z, stats, params[layer], ups, states, slopes)
        sums = gather_sums(sums)
        grad_z, sent, sums = norm_back(
            other_columns, place, grad_pre, z, stats, params[layer], sums, valid, weight, layer
        )
        received = swap_half(sent)
        leaving = jnp.concatenate(
            [grad_z[:, width : 2 * width], grad_z[:, 3 * width :]], axis=1
        )
        halves = weight_terms(lists, place, grad_z, swap(leaving, 1), groups)
        kept = own_terms(own_columns, place, after(grad_z, halves[0]), ups, weight, layer)
        ups = [kept, received]
        shares = []
        for half, axes in enumerate((("x", "y"), ("y", "x"))):
            total = halves[2 * half] + lax.ppermute(halves[2 * half + 1], axes[0], FLIP2)
            total = total[0] + lax.ppermute(total[1], axes[1], FLIP2)
            shares.append(total[0] + lax.ppermute(total[1], "h", FLIP2))
        grad_weights = assemble(y_x, *plane_gather(*shares), layer, grad_weights)
        sums = lax.dynamic_index_in_dim(sums.reshape(3, 4, width), clip, axis=1, keepdims=False)
        results[layer] = sums
    grad_in = ups[0] + ups[1]
    grad_in = [swap(grad_in[:, r * width : (r + 1) * width], r) for r in range(4)]
    sums = jnp.stack(results)
    return (
        unpack(place, output),
        unpack(place, grad_in),
        grad_weights,
        sums[:, 0],
        sums[:, 1],
        sums[:, 2],
        sums[:, 1],
    )


def gelu_slope(value):
    return (
        0.5 * (1.0 + jax.scipy.special.erf(value / ROOT_TWO))
        + value * jnp.exp(-0.5 * value * value) / ROOT_TWO_PI
    )


def recur_step(decay, state, inputs):
    drive_t, valid_t = inputs
    pre = drive_t + decay * state
    state = state + valid_t * (jax.nn.gelu(pre, approximate=False) - state)
    return (state, state)


def back_step(decay, carry, inputs):
    upstream_t, valid_t, pre_t = inputs
    total = upstream_t + carry
    grad_pre = total * valid_t * gelu_slope(pre_t)
    carry = total * (1.0 - valid_t) + grad_pre * decay
    return (carry, grad_pre)


def add_piece(weight, piece):
    return jnp.dot(weight, piece, precision=HIGH, preferred_element_type=jnp.float32)


def weight_columns(grad_pre_norm, piece):
    return jnp.einsum("jf,kf->jk", grad_pre_norm, piece, precision=HIGH)


def split_features(inputs, weights, gains, shifts, decays, biases, lengths, frame_mask, grad_out):
    width, slots = inputs.shape
    clips, frames_len = frame_mask.shape
    frames = jnp.arange(frames_len, dtype=jnp.int32)
    valid_grid = (
        (frames[None, :] < lengths[:, None]) & ((frame_mask == 1) | (frames[None, :] == 0))
    ).astype(jnp.float32)
    valid = valid_grid.reshape(-1)
    valid_row = valid[None, :]
    valid_time = jnp.broadcast_to(valid_grid.T[:, :, None], (frames_len, clips, width)).reshape(
        frames_len, clips * width
    )
    count_local = jnp.sum(valid)

    def to_time(array):
        return jnp.transpose(array.reshape(width, clips, frames_len), (2, 1, 0)).reshape(
            frames_len, clips * width
        )

    def from_time(array):
        return jnp.transpose(array.reshape(frames_len, clips, width), (2, 1, 0)).reshape(
            width, slots
        )

    layer_in = inputs
    saved = []
    for layer_no in range(LAYERS):
        weight = weights[layer_no]
        gathered = lax.all_gather(layer_in, "neuron", axis=0, tiled=True)
        pre_norm = add_piece(weight, gathered)
        first_sum, count = lax.psum((jnp.sum(valid_row * pre_norm, axis=1), count_local), "batch")
        mean = first_sum / count
        centered = pre_norm - mean[:, None]
        var = lax.psum(jnp.sum(valid_row * centered * centered, axis=1), "batch") / count
        inv_std = lax.rsqrt(var + EPS)
        zhat = (pre_norm - mean[:, None]) * inv_std[:, None]
        drive = gains[layer_no][:, None] * zhat + (shifts[layer_no] + biases[layer_no])[:, None]
        drive_time = to_time(drive)
        decay_wide = jnp.tile(decays[layer_no], clips)
        start_state = jnp.zeros((clips * width,), jnp.float32)
        _, states = lax.scan(
            partial(recur_step, decay_wide), start_state, (drive_time, valid_time), unroll=8
        )
        saved.append((gathered, zhat, inv_std, drive_time, states, count))
        layer_in = layer_in + valid_row * from_time(states)
    upstream = grad_out
    grad_parts = [None] * LAYERS
    for layer_no in range(LAYERS - 1, -1, -1):
        gathered, zhat, inv_std, drive_time, states, count = saved[layer_no]
        decay_wide = jnp.tile(decays[layer_no], clips)
        gain = gains[layer_no]
        previous = jnp.concatenate([jnp.zeros_like(states[:1]), states[:-1]], axis=0)
        pre_time = drive_time + decay_wide[None, :] * previous
        grad_state = to_time(valid_row * upstream)
        start_carry = jnp.zeros((clips * width,), jnp.float32)
        _, grad_pre_time = lax.scan(
            partial(back_step, decay_wide),
            start_carry,
            (grad_state, valid_time, pre_time),
            reverse=True,
            unroll=8,
        )
        decay_local = jnp.sum(
            jnp.sum(grad_pre_time * previous, axis=0).reshape(clips, width), axis=0
        )
        grad_pre = from_time(grad_pre_time)
        gain_local = jnp.sum(grad_pre * zhat, axis=1)
        shift_local = jnp.sum(grad_pre, axis=1)
        grad_gain, grad_shift, grad_decay = lax.psum(
            (gain_local, shift_local, decay_local), "batch"
        )
        grad_pre_norm = (gain * inv_std)[:, None] * (
            grad_pre - valid_row * (grad_shift[:, None] + zhat * grad_gain[:, None]) / count
        )
        weight_local = weight_columns(grad_pre_norm, gathered)
        input_terms = jnp.einsum("jk,jf->kf", weights[layer_no], grad_pre_norm, precision=HIGH)
        input_grad = lax.psum_scatter(input_terms, "neuron", scatter_dimension=0, tiled=True)
        grad_weight = lax.psum(weight_local, "batch")
        upstream = upstream + input_grad
        grad_parts[layer_no] = (grad_weight, grad_gain, grad_shift, grad_decay)
    grad_weights = jnp.stack([grad_parts[layer_no][0] for layer_no in range(LAYERS)])
    grad_gains = jnp.stack([grad_parts[layer_no][1] for layer_no in range(LAYERS)])
    grad_shifts = jnp.stack([grad_parts[layer_no][2] for layer_no in range(LAYERS)])
    grad_decays = jnp.stack([grad_parts[layer_no][3] for layer_no in range(LAYERS)])
    return (layer_in, upstream, grad_weights, grad_gains, grad_shifts, grad_decays, grad_shifts)


def solution(mesh):
    if (mesh.shape["batch"], mesh.shape["neuron"]) == (4, 8):
        cut = Mesh(mesh.devices.reshape(2, 2, 2, 2, 2), ("y", "x", "h", "l", "c"))
        batch, neuron, body = ("y", "x"), ("h", "l", "c"), half_features
    else:
        cut, batch, neuron, body = mesh, "batch", "neuron", split_features
    in_specs = (
        P(neuron, batch),
        P(None, neuron, None),
        P(None, neuron),
        P(None, neuron),
        P(None, neuron),
        P(None, neuron),
        P(batch),
        P(batch, None),
        P(neuron, batch),
    )
    out_specs = (
        P(neuron, batch),
        P(neuron, batch),
        P(None, neuron, None),
        P(None, neuron),
        P(None, neuron),
        P(None, neuron),
        P(None, neuron),
    )
    return jax.shard_map(
        body, mesh=cut, in_specs=in_specs, out_specs=out_specs, check_vma=False
    )
```

```python
from functools import partial
import math

import jax
import jax.numpy as jnp
from jax import lax
from jax.experimental import pallas as pl
from jax.experimental.pallas import tpu as pltpu
from jax.sharding import Mesh, PartitionSpec as P

LAYERS = 2
EPS = 1e-05
HIGH = lax.Precision.HIGHEST
ROOT_TWO = math.sqrt(2.0)
ROOT_TWO_PI = math.sqrt(2.0 * math.pi)
F32 = jnp.float32
BF16 = jnp.bfloat16
LANES = 128
VMEM_LIMIT = 48 * 1024 * 1024
SMEM_SPEC = pl.BlockSpec(memory_space=pltpu.SMEM)
VMEM_SPEC = pl.BlockSpec(memory_space=pltpu.VMEM)


FLIP2 = [(0, 1), (1, 0)]


def flip_of(rel):
    if rel == 1:
        return "c", FLIP2
    if rel == 2:
        return "h", FLIP2
    return ("h", "c"), [(i, i ^ 3) for i in range(4)]


def swap(array, rel):
    if rel == 0:
        return array
    axes, pairs = flip_of(rel)
    return lax.ppermute(array, axes, pairs)


def swap_half(array):
    return lax.ppermute(array, "l", FLIP2)


def split(value):
    high = value.astype(BF16)
    return high, (value - high.astype(F32)).astype(BF16)


def dot(a, b, dims):
    return lax.dot_general(a, b, (dims, ((), ())), preferred_element_type=F32)


NT = ((1,), (1,))
NN = ((1,), (0,))


def call(body, **kwargs):
    return pl.pallas_call(
        body,
        compiler_params=pltpu.CompilerParams(vmem_limit_bytes=VMEM_LIMIT),
        **kwargs,
    )


def cost(flops, byte_count):
    return pl.CostEstimate(flops=int(flops) // 64, bytes_accessed=int(byte_count) // 64, transcendentals=0)


def pack_body(frames, place_ref, in_ref, *refs):
    outs, turned = refs[:4], refs[4]
    slots = in_ref.shape[1]
    for start in range(0, slots, LANES):
        turned[start : start + LANES, :] = in_ref[:, start : start + LANES].T
    for rel in range(4):
        first = pl.multiple_of(place_ref[rel] * frames, 8)
        outs[rel][...] = turned[pl.ds(first, frames), :]


def pack(place, array, frames):
    width, slots = array.shape
    return call(
        partial(pack_body, frames),
        out_shape=[jax.ShapeDtypeStruct((frames, width), F32)] * 4,
        in_specs=[SMEM_SPEC, VMEM_SPEC],
        out_specs=[VMEM_SPEC] * 4,
        scratch_shapes=[pltpu.VMEM((slots, width), F32)],
        cost_estimate=cost(0, 8 * width * slots),
        name="pack",
    )(place, array)


def unpack_body(frames, place_ref, *refs):
    ins, out_ref, turned = refs[:4], refs[4], refs[5]
    slots = out_ref.shape[1]
    for rel in range(4):
        first = pl.multiple_of(place_ref[rel] * frames, 8)
        turned[pl.ds(first, frames), :] = ins[rel][...]
    for start in range(0, slots, LANES):
        out_ref[:, start : start + LANES] = turned[start : start + LANES, :].T


def unpack(place, pieces):
    frames, width = pieces[0].shape
    slots = 4 * frames
    return call(
        partial(unpack_body, frames),
        out_shape=jax.ShapeDtypeStruct((width, slots), F32),
        in_specs=[SMEM_SPEC] + [VMEM_SPEC] * 4,
        out_specs=VMEM_SPEC,
        scratch_shapes=[pltpu.VMEM((slots, width), F32)],
        cost_estimate=cost(0, 8 * width * slots),
        name="unpack",
    )(place, *pieces)


def spread_of(parts, width):
    spots, row, column = [], 0, 0
    for part in parts:
        spots.append((row, column))
        if part.shape[1] == width:
            column += width
        else:
            row += part.shape[0]
    return spots


def project_body(n_parts, spots, with_acc, with_stats, flat, cols_ref, place_ref, *refs):
    del cols_ref
    parts, refs = refs[:n_parts], refs[n_parts:]
    weights, refs = refs[:4], refs[4:]
    if with_acc:
        acc_ref, refs = refs[0], refs[1:]
    if with_stats:
        valid_ref, refs = refs[0], refs[1:]
    out_ref, refs = refs[0], refs[1:]
    if with_stats:
        stats_ref, refs = refs[0], refs[1:]
    if flat:
        flat_ref, refs = refs[0], refs[1:]
    x_high, x_low = refs
    step = pl.program_id(0)
    width = x_high.shape[2]

    @pl.when(step == 0)
    def _():
        for (row, column), part in zip(spots, parts):
            rows, columns = part.shape
            for start in range(0, columns, width):
                rel = (column + start) // width
                high, low = split(part[:, start : start + width])
                x_high[rel, row : row + rows, :] = high
                x_low[rel, row : row + rows, :] = low
            if flat:
                flat_ref[row : row + rows, column : column + columns] = part[...]
        if with_acc:
            out_ref[...] = acc_ref[...]
        else:
            out_ref[...] = jnp.zeros_like(out_ref)

    stacked = jnp.concatenate([x_high[step], x_low[step], x_high[step]], axis=1)
    for block in range(4):
        w_high, w_low = split(weights[block][...].reshape(width, width))
        columns = slice(block * width, (block + 1) * width)
        out_ref[:, columns] += dot(stacked, jnp.concatenate([w_high, w_high, w_low], axis=1), NT)

    if with_stats:

        @pl.when(step == pl.num_programs(0) - 1)
        def _():
            valid = valid_ref[...]
            own = jnp.sum(valid, axis=0, keepdims=True)
            per = width // LANES
            for row in range(out_ref.shape[1] // LANES):
                z = out_ref[:, row * LANES : (row + 1) * LANES]
                total = jnp.sum(valid * z, axis=0, keepdims=True)
                centred = valid * (z - total / own)
                squares = jnp.sum(centred * centred, axis=0, keepdims=True)
                at = place_ref[row // per] * per + row % per
                stats_ref[0, pl.ds(at, 1), :] = total
                stats_ref[1, pl.ds(at, 1), :] = squares
                stats_ref[2, pl.ds(at, 1), :] = own


def weight_specs(weights, layer, pairs=2):
    specs = []
    for weight in weights:
        width = weight.shape[-2]
        if weight.ndim == 3:
            specs.append(
                pl.BlockSpec((1, width, pairs * width), lambda s, cols, *_: (layer, 0, cols[s]))
            )
        else:
            specs.append(pl.BlockSpec((width, pairs * width), lambda s, cols, *_: (0, cols[s])))
    return specs


def project(columns, place, parts, weights, layer, acc=None, valid=None, flat=False):
    width = weights[0].shape[-2]
    frames = sum(p.shape[0] for p in parts if p.shape[1] != width) or parts[0].shape[0]
    full = pl.BlockSpec(memory_space=pltpu.VMEM)
    in_specs = [full] * len(parts)
    in_specs += weight_specs(weights, layer, 1)
    operands = list(parts) + list(weights)
    array = jax.ShapeDtypeStruct((frames, 4 * width), F32)
    array_spec = pl.BlockSpec((frames, 4 * width), lambda s, cols, place: (0, 0))
    out_shape, out_specs = [array], [array_spec]
    if acc is not None:
        in_specs.append(full)
        operands.append(acc)
    if valid is not None:
        in_specs.append(full)
        operands.append(valid)
        rows = 4 * width // LANES
        out_shape.append(jax.ShapeDtypeStruct((3, rows, LANES), F32))
        out_specs.append(pl.BlockSpec((3, rows, LANES), lambda s, cols, place: (0, 0, 0)))
    if flat:
        out_shape.append(array)
        out_specs.append(array_spec)
    return call(
        partial(
            project_body,
            len(parts),
            spread_of(parts, width),
            acc is not None,
            valid is not None,
            flat,
        ),
        grid_spec=pltpu.PrefetchScalarGridSpec(
            num_scalar_prefetch=2,
            grid=(4,),
            in_specs=in_specs,
            out_specs=out_specs,
            scratch_shapes=[pltpu.VMEM((4, frames, width), BF16)] * 2,
        ),
        out_shape=out_shape,
        cost_estimate=cost(2 * 3 * frames * 16 * width * width, 4 * 16 * width * width),
        name="project",
    )(columns, place, *operands)


def to_relative(place_ref, spread, rows_ref, value, slot):
    per = value.shape[0] // 4
    spread[...] = value
    for rel in range(4):
        first = place_ref[rel] * per
        for row in range(per):
            rows_ref[slot, rel * per + row : rel * per + row + 1, :] = spread[
                pl.ds(first + row, 1), :
            ]


def tree(values):
    while len(values) > 1:
        values = [a + b for a, b in zip(values[::2], values[1::2])]
    return values[0]


def norm_terms(stats_refs):
    each = [[ref[i, slot] for ref in stats_refs for i in range(4)] for slot in range(3)]
    totals, squares, owns = each
    count = tree(owns)
    mean = tree(totals) / count
    away = [total / own - mean for total, own in zip(totals, owns)]
    spread = tree([s + n * a * a for s, n, a in zip(squares, owns, away)])
    return count, mean, lax.rsqrt(spread / count + EPS)


def recur_body(n_parts, spots, out_cols, first, place_ref, gate_ref, z_ref, s0, s1, s2, s3, params_ref, valid_ref, start_ref, *refs):
    parts, refs = refs[:n_parts], refs[n_parts:]
    n_out = len(out_cols)
    outs, refs = refs[:n_out], refs[n_out:]
    state_ref, slope_ref, last_ref, rows, spread, drive_s, state_s, slope_s = refs
    frames = z_ref.shape[0]
    blocks = z_ref.shape[1] // LANES
    _, mean, inv_std = norm_terms((s0, s1, s2, s3))
    to_relative(place_ref, spread, rows, mean, 0)
    to_relative(place_ref, spread, rows, params_ref[0] * inv_std, 1)
    to_relative(place_ref, spread, rows, params_ref[1], 2)
    to_relative(place_ref, spread, rows, params_ref[2], 3)
    for row in range(blocks):
        z = z_ref[:, row * LANES : (row + 1) * LANES]
        drive_s[row * frames : (row + 1) * frames, :] = (
            z - rows[0, row : row + 1, :]
        ) * rows[1, row : row + 1, :] + rows[2, row : row + 1, :]
    decay = rows[3]

    def step(t, state):
        at = pl.ds(t, blocks, stride=frames)
        pre = drive_s[at, :] + decay * state
        half = 0.5 + 0.5 * lax.erf(pre * (1.0 / ROOT_TWO))
        gate = gate_ref[first + t] > 0.0
        slope = half + pre * jnp.exp(-0.5 * pre * pre) * (1.0 / ROOT_TWO_PI)
        state = jnp.where(gate, pre * half, state)
        state_s[at, :] = state
        slope_s[at, :] = jnp.where(gate, slope, 0.0)
        return state

    last_ref[...] = lax.fori_loop(0, frames, step, start_ref[...], unroll=8)
    valid = valid_ref[...]
    for row in range(blocks):
        lanes = slice(row * LANES, (row + 1) * LANES)
        state = state_s[row * frames : (row + 1) * frames, :]
        state_ref[:, lanes] = state
        slope_ref[:, lanes] = slope_s[row * frames : (row + 1) * frames, :]
        for (top, column), part in zip(spots, parts):
            if column <= row * LANES < column + part.shape[1]:
                x = part[:, row * LANES - column : (row + 1) * LANES - column]
                some = slice(top, top + part.shape[0])
                for out_column, out in zip(out_cols, outs):
                    if out_column <= row * LANES < out_column + out.shape[1]:
                        at = row * LANES - out_column
                        out[some, at : at + LANES] = x + valid[some] * state[some]


def recur(chunk, chunks, place, gate, z, stats, params, valid, start, parts, pieces):
    frames = z.shape[0] // chunks
    features = z.shape[1]
    width = features // 4
    blocks = features // LANES
    row_block = lambda columns: pl.BlockSpec((frames, columns), lambda i: (chunk, 0))
    whole = lambda array: pl.BlockSpec(array.shape, lambda i: (0,) * array.ndim)
    part_specs = [row_block(p.shape[1]) if p.shape[0] == z.shape[0] else whole(p) for p in parts]
    n_out = pieces
    out_width = features // n_out
    tile = jax.ShapeDtypeStruct((blocks, LANES), F32)
    full = jax.ShapeDtypeStruct((frames, features), F32)
    out_shape = [jax.ShapeDtypeStruct((frames, out_width), F32)] * n_out + [full, full, tile]
    return call(
        partial(
            recur_body,
            len(parts),
            spread_of(parts, width),
            [i * out_width for i in range(n_out)],
            chunk * frames,
        ),
        grid=(1,),
        in_specs=[
            SMEM_SPEC,
            SMEM_SPEC,
            row_block(features),
            *[whole(s) for s in stats],
            whole(params),
            row_block(LANES),
            whole(start),
        ]
        + part_specs,
        out_specs=[whole(s) for s in out_shape],
        out_shape=out_shape,
        scratch_shapes=[
            pltpu.VMEM((4, blocks, LANES), F32),
            pltpu.VMEM((blocks, LANES), F32),
        ]
        + [pltpu.VMEM((blocks * frames, LANES), F32)] * 3,
        cost_estimate=cost(100 * frames * features, 20 * frames * features),
        name="recur",
    )(place, gate, z, *stats, params, valid, start, *parts)


def back_body(n_parts, spots, n_state, place_ref, gate_ref, z_ref, s0, s1, s2, s3, params_ref, *refs):
    parts, refs = refs[:n_parts], refs[n_parts:]
    states, refs = refs[:n_state], refs[n_state:]
    slopes, refs = refs[:n_state], refs[n_state:]
    grad_ref, sums_ref, rows, spread, up_s, state_s, slope_s = refs
    frames = z_ref.shape[0]
    blocks = z_ref.shape[1] // LANES
    tall = frames + 8
    _, mean, inv_std = norm_terms((s0, s1, s2, s3))
    to_relative(place_ref, spread, rows, mean, 0)
    to_relative(place_ref, spread, rows, inv_std, 1)
    to_relative(place_ref, spread, rows, params_ref[2], 2)
    for row in range(blocks):
        lanes = slice(row * LANES, (row + 1) * LANES)
        base = row * frames
        up = None
        for (top, column), part in zip(spots, parts):
            if column <= row * LANES < column + part.shape[1] and part.shape[0] == frames:
                value = part[:, row * LANES - column : (row + 1) * LANES - column]
                up = value if up is None else up + value
        up_s[base : base + frames, :] = up
        state_s[row * tall : row * tall + 8, :] = jnp.zeros((8, LANES), F32)
        first = 0
        for state, slope in zip(states, slopes):
            some = state.shape[0]
            at = row * tall + 8 + first
            state_s[at : at + some, :] = state[:, lanes]
            slope_s[base + first : base + first + some, :] = slope[:, lanes]
            first += some
    decay = rows[2]

    def step(i, carry):
        t = frames - 1 - i
        at = pl.ds(t, blocks, stride=frames)
        slope = slope_s[at, :]
        gate = gate_ref[t]
        total = gate * up_s[at, :] + carry
        up_s[at, :] = total * slope
        return total * (slope * decay + (1.0 - gate))

    lax.fori_loop(0, frames, step, jnp.zeros((blocks, LANES), F32), unroll=8)
    per = blocks // 4
    for row in range(blocks):
        lanes = slice(row * LANES, (row + 1) * LANES)
        base = row * frames
        grad = up_s[base : base + frames, :]
        grad_ref[:, lanes] = grad
        zhat = (z_ref[:, lanes] - rows[0, row : row + 1, :]) * rows[1, row : row + 1, :]
        before = state_s[row * tall + 7 : row * tall + 7 + frames, :]
        at = place_ref[row // per] * per + row % per
        for slot, value in enumerate((grad * zhat, grad, grad * before)):
            sums_ref[slot, pl.ds(at, 1), :] = jnp.sum(value, axis=0, keepdims=True)


def spots_of_sum(parts, width):
    spots, column = [], 0
    for part in parts:
        spots.append((0, column % (4 * width)))
        column += part.shape[1]
    return spots


def back(place, gate, z, stats, params, ups, states, slopes):
    frames, features = z.shape
    width = features // 4
    blocks = features // LANES
    return call(
        partial(back_body, len(ups), spots_of_sum(ups, width), len(states)),
        in_specs=[SMEM_SPEC] * 2 + [VMEM_SPEC] * (6 + len(ups) + 2 * len(states)),
        out_specs=[VMEM_SPEC] * 2,
        out_shape=[
            jax.ShapeDtypeStruct((frames, features), F32),
            jax.ShapeDtypeStruct((3, blocks, LANES), F32),
        ],
        scratch_shapes=[
            pltpu.VMEM((3, blocks, LANES), F32),
            pltpu.VMEM((blocks, LANES), F32),
            pltpu.VMEM((blocks * frames, LANES), F32),
            pltpu.VMEM((blocks * (frames + 8), LANES), F32),
            pltpu.VMEM((blocks * frames, LANES), F32),
        ],
        cost_estimate=cost(30 * frames * features, 20 * frames * features),
        name="back",
    )(place, gate, z, *stats, params, *ups, *states, *slopes)


def input_terms(high_s, low_s, weights):
    width = high_s.shape[2]
    left, right = [], []
    for block, weight in enumerate(weights):
        w_high, w_low = split(weight[...].reshape(width, 2 * width))
        left += [high_s[block], low_s[block], high_s[block]]
        right += [w_high, w_high, w_low]
    return dot(jnp.concatenate(left, axis=1), jnp.concatenate(right, axis=0), NN)


def norm_back_body(cols_ref, place_ref, grad_ref, z_ref, params_ref, valid_ref, *refs):
    del cols_ref
    stats_refs, sums_refs, refs = refs[:4], refs[4:8], refs[8:]
    weights, refs = refs[:4], refs[4:]
    out_ref, near_term_ref, far_term_ref, sums_out_ref, rows, spread, high_s, low_s = refs
    blocks = z_ref.shape[1] // LANES
    width = high_s.shape[2]
    per = width // LANES

    @pl.when(pl.program_id(0) == 0)
    def _():
        count, mean, inv_std = norm_terms(stats_refs)
        to_relative(place_ref, spread, rows, mean, 0)
        to_relative(place_ref, spread, rows, inv_std, 1)
        to_relative(place_ref, spread, rows, params_ref[0] * inv_std, 2)
        sums = tree([ref[...] for ref in sums_refs])
        sums_out_ref[...] = sums
        to_relative(place_ref, spread, rows, sums[0] / count, 3)
        to_relative(place_ref, spread, rows, sums[1] / count, 4)
        valid = valid_ref[...]
        for row in range(blocks):
            lanes = slice(row * LANES, (row + 1) * LANES)
            one = lambda slot: rows[slot, row : row + 1, :]
            zhat = (z_ref[:, lanes] - one(0)) * one(1)
            value = one(2) * (grad_ref[:, lanes] - valid * (one(4) + zhat * one(3)))
            out_ref[:, lanes] = value
            high, low = split(value)
            inner = slice((row % per) * LANES, (row % per + 1) * LANES)
            high_s[row // per, :, inner] = high
            low_s[row // per, :, inner] = low

    value = input_terms(high_s, low_s, weights)
    for step, term_ref in enumerate((far_term_ref, near_term_ref)):

        @pl.when(pl.program_id(0) == step)
        def _():
            for pair in range(2):
                at = pl.multiple_of(((place_ref[0] & 1) ^ pair) * width, width)
                term_ref[:, pl.ds(at, width)] = value[:, pair * width : (pair + 1) * width]


def norm_back(columns, place, grad, z, params, valid, stats, sums, weights, layer):
    frames, features = z.shape
    width = features // 4
    blocks = features // LANES
    whole = lambda array: pl.BlockSpec(array.shape, lambda s, cols, place: (0,) * array.ndim)
    operands = [grad, z, params, valid, *stats, *sums]
    full = jax.ShapeDtypeStruct((frames, features), F32)
    half = jax.ShapeDtypeStruct((frames, 2 * width), F32)
    out_shape = [full, half, half, jax.ShapeDtypeStruct((3, blocks, LANES), F32)]
    return call(
        norm_back_body,
        grid_spec=pltpu.PrefetchScalarGridSpec(
            num_scalar_prefetch=2,
            grid=(2,),
            in_specs=[whole(a) for a in operands] + weight_specs(weights, layer),
            out_specs=[whole(a) for a in out_shape],
            scratch_shapes=[
                pltpu.VMEM((5, blocks, LANES), F32),
                pltpu.VMEM((blocks, LANES), F32),
                pltpu.VMEM((4, frames, width), BF16),
                pltpu.VMEM((4, frames, width), BF16),
            ],
        ),
        out_shape=out_shape,
        cost_estimate=cost(6 * frames * features * features, 4 * features * features),
        name="norm_back",
    )(columns[::-1], place, *operands, *weights)


def own_terms_body(n_ups, spots, cols_ref, place_ref, grad_ref, *refs):
    del cols_ref
    ups, refs = refs[:n_ups], refs[n_ups:]
    weights, refs = refs[:4], refs[4:]
    out_ref, high_s, low_s = refs
    width = high_s.shape[2]
    step = pl.program_id(0)

    @pl.when(step == 0)
    def _():
        for block in range(4):
            high, low = split(grad_ref[:, block * width : (block + 1) * width])
            high_s[block] = high
            low_s[block] = low

    value = input_terms(high_s, low_s, weights)
    for pair in range(2):
        at = pl.multiple_of(((place_ref[0] & 1) ^ pair) * width, width)
        out_ref[:, pl.ds(at, width)] = value[:, pair * width : (pair + 1) * width]
    for half in range(2):

        @pl.when(step == half)
        def _():
            first = 2 * half * width
            for (_, column), up in zip(spots, ups):
                low = max(column, first)
                high = min(column + up.shape[1], first + 2 * width)
                if low < high:
                    out_ref[:, low - first : high - first] += up[:, low - column : high - column]


def own_terms(columns, place, grad, ups, weights, layer):
    frames, features = grad.shape
    width = features // 4
    whole = lambda array: pl.BlockSpec(array.shape, lambda s, cols, place: (0,) * array.ndim)
    step_block = pl.BlockSpec((frames, 2 * width), lambda s, cols, place: (0, s))
    return call(
        partial(own_terms_body, len(ups), spots_of_sum(ups, width)),
        grid_spec=pltpu.PrefetchScalarGridSpec(
            num_scalar_prefetch=2,
            grid=(2,),
            in_specs=[whole(a) for a in (grad, *ups)]
            + weight_specs(weights, layer),
            out_specs=step_block,
            scratch_shapes=[pltpu.VMEM((4, frames, width), BF16)] * 2,
        ),
        out_shape=jax.ShapeDtypeStruct((frames, features), F32),
        cost_estimate=cost(6 * frames * features * features, 4 * features * features),
        name="own_terms",
    )(columns, place, grad, *ups, *weights)


def weight_body(half, n_chunks, lists_ref, place_ref, *refs):
    del lists_ref
    if half == 0:
        grad_ref, near_ref, refs = refs[0], refs[1], refs[2:]
    else:
        turned, refs = refs[0], refs[1:]
    per_group = []
    for _ in range(4):
        per_group.append(refs[:n_chunks])
        refs = refs[n_chunks:]
    kept, sent, refs = refs[0], refs[1], refs[2:]
    if half == 0:
        turned, refs = refs[0], refs[1:]
    ordered, x_all = refs
    step = pl.program_id(0)
    width = x_all.shape[1]
    padded = x_all.shape[0] // 6
    rows = width // 4

    @pl.when(step == 0)
    def _():
        x_all[...] = jnp.zeros_like(x_all)
        if half == 0:
            frames = grad_ref.shape[0]
            turned[...] = jnp.zeros_like(turned)
            for clip in range(2):
                for dh in range(2):
                    if clip == 0:
                        part = grad_ref[:, 2 * dh * width : (2 * dh + 1) * width]
                    else:
                        part = near_ref[:, dh * width : (dh + 1) * width]
                    high, low = split(part.T)
                    for slot, value in enumerate((high, high, low)):
                        first = (3 * clip + slot) * padded
                        turned[dh * width : (dh + 1) * width, first : first + frames] = value
        for i in range(4):
            for dh in range(2):
                dy, dx = (i % 2, i // 2) if half == 0 else (i // 2, i % 2)
                y, x = place_ref[4] ^ dy, place_ref[5] ^ dx
                at = pl.multiple_of(dh * width + (2 * y + x) * rows, rows)
                to = (2 * i + dh) * rows
                ordered[to : to + rows, :] = turned[pl.ds(at, rows), :]

    for side in range(2):

        @pl.when(step // 2 == side)
        def _():
            for clip in range(2):
                row = 0
                for part in per_group[2 * clip + side]:
                    some = part.shape[0]
                    high, low = split(part[...])
                    for slot, value in enumerate((high, low, high)):
                        first = (3 * clip + slot) * padded + row
                        x_all[first : first + some, :] = value
                    row += some

    value = dot(ordered[...], x_all[...], NN)
    kept[...] = value[:width].reshape(kept.shape)
    sent[...] = value[width:].reshape(sent.shape)


def weight_terms(half, lists, place, turned, groups):
    width = groups[0][0].shape[1] // 4
    frames = sum(part.shape[0] for part in groups[0])
    padded = -(-frames // LANES) * LANES
    whole = lambda array: pl.BlockSpec(array.shape, lambda s, src, place: (0,) * array.ndim)
    operands = list(turned)
    in_specs = [whole(a) for a in operands]
    for i, group in enumerate(groups):
        for part in group:
            operands.append(part)
            at = 8 * (i // 2) + 4 * half
            in_specs.append(
                pl.BlockSpec(
                    (part.shape[0], width), lambda s, src, place, at=at: (0, src[at + s])
                )
            )
    shape = (2, 2, width // 4, 4 * width)
    at = 16 + 4 * half
    out_specs = [
        pl.BlockSpec(shape[:3] + (width,), lambda s, src, place: (0, 0, 0, src[at + s]))
    ] * 2
    out_shape = [jax.ShapeDtypeStruct(shape, F32)] * 2
    if half == 0:
        out_shape.append(jax.ShapeDtypeStruct((2 * width, 6 * padded), BF16))
        out_specs.append(whole(out_shape[-1]))
    return call(
        partial(weight_body, half, len(groups[0])),
        grid_spec=pltpu.PrefetchScalarGridSpec(
            num_scalar_prefetch=2,
            grid=(4,),
            in_specs=in_specs,
            out_specs=out_specs,
            scratch_shapes=[
                pltpu.VMEM((2 * width, 6 * padded), BF16),
                pltpu.VMEM((6 * padded, width), BF16),
            ],
        ),
        out_shape=out_shape,
        cost_estimate=cost(12 * frames * 2 * width * 4 * width, 4 * 8 * width * width),
        name="weight_terms",
    )(lists, place, *operands)


def plane_gather(first, second=None):
    if second is None:
        half = first.shape[1] // 2
        first, second = first[:, :half], first[:, half:]
    first = [first, lax.ppermute(first, "x", FLIP2)]
    second = [second, lax.ppermute(second, "y", FLIP2)]
    first += [lax.ppermute(piece, "y", FLIP2) for piece in first]
    second += [lax.ppermute(piece, "x", FLIP2) for piece in second]
    second = [second[0], second[2], second[1], second[3]]
    return first, second


def keep_body(in_ref, out_ref):
    out_ref[0] = in_ref[...]


def keep(array, layer):
    return call(
        keep_body,
        grid=(1,),
        out_shape=jax.ShapeDtypeStruct((LAYERS, *array.shape), F32),
        in_specs=[pl.BlockSpec(array.shape, lambda i: (0, 0))],
        out_specs=pl.BlockSpec((1, *array.shape), lambda i: (layer, 0, 0)),
        cost_estimate=cost(0, 8 * array.size),
        name="keep",
    )(array)


def assemble_body(y_x_ref, *refs):
    first, second, out_ref = refs[:4], refs[4:8], refs[-1]
    rows, half = first[0].shape
    for rel in range(4):
        at = pl.multiple_of(
            (2 * (y_x_ref[0] ^ (rel // 2)) + (y_x_ref[1] ^ (rel % 2))) * rows, rows
        )
        out_ref[..., pl.ds(at, rows), :half] = first[rel][...].reshape(
            out_ref.shape[:-2] + (rows, half)
        )
        out_ref[..., pl.ds(at, rows), half:] = second[rel][...].reshape(
            out_ref.shape[:-2] + (rows, half)
        )


def assemble(y_x, first, second, layer=None, onto=None):
    rows, half = first[0].shape
    shape = (4 * rows, 2 * half)
    out_spec, aliases, extra, extra_specs = VMEM_SPEC, {}, [], []
    if layer is not None:
        out_spec = pl.BlockSpec((1, *shape), lambda i: (layer, 0, 0))
        if onto is not None:
            aliases, extra = {9: 0}, [onto]
            extra_specs = [pl.BlockSpec(memory_space=pl.ANY)]
        shape = (LAYERS, *shape)
    whole = pl.BlockSpec((rows, half), lambda i: (0, 0))
    return call(
        assemble_body,
        grid=(1,),
        out_shape=jax.ShapeDtypeStruct(shape, F32),
        in_specs=[SMEM_SPEC] + [whole] * 8 + extra_specs,
        out_specs=out_spec if layer is not None else pl.BlockSpec(shape, lambda i: (0, 0)),
        input_output_aliases=aliases,
        cost_estimate=cost(0, 8 * rows * half * 8),
        name="assemble",
    )(y_x, *first, *second, *extra)


def after(value, *others):
    return lax.optimization_barrier((value, others))[0]


def half_features(inputs, weights, gains, shifts, decays, biases, lengths, frame_mask, grad_out):
    width, slots = inputs.shape
    clips, frames = frame_mask.shape
    depth = weights.shape[2]
    blocks = 4 * width // LANES
    y, x, h, l, c = (lax.axis_index(name) for name in ("y", "x", "h", "l", "c"))
    b = 2 * y + x
    numbers = [2 * (h ^ (rel // 2)) + (c ^ (rel % 2)) for rel in range(4)] + [y, x]
    place = jnp.stack(numbers).astype(jnp.int32)
    own_blocks, other_blocks = (
        jnp.stack(
            [2 * (2 * (h ^ (rel // 2)) + half) + (c ^ (rel % 2)) for rel in range(4)]
        ).astype(jnp.int32)
        for half in (l, 1 - l)
    )
    own_columns = jnp.stack([2 * h + l, 2 * (1 - h) + l]).astype(jnp.int32)
    other_columns = jnp.stack([2 * h + 1 - l, 2 * (1 - h) + 1 - l]).astype(jnp.int32)
    mine, theirs, spots = [], [], []
    for at_h in range(2):
        for dl in range(2):
            for dc in range(2):
                mine.append(2 * (h ^ at_h) + dc)
                theirs.append(2 * (h ^ at_h) + (1 - dc))
                spots.append(2 * (l ^ dl) + (c ^ dc))
    lists = jnp.stack(mine + theirs + spots).astype(jnp.int32)
    y_x = place[4:]
    rows = width // 4

    clip = 2 * h + c
    seen = lax.dynamic_index_in_dim(frame_mask, clip, 0, keepdims=False)
    length = lax.dynamic_index_in_dim(lengths, clip, 0, keepdims=False)
    moments = jnp.arange(frames, dtype=jnp.int32)
    gate = ((moments < length) & ((seen == 1) | (moments == 0))).astype(F32)
    valid = jnp.broadcast_to(gate[:, None], (frames, LANES))

    params = jnp.stack([gains, shifts + biases, decays], axis=1).reshape(LAYERS, 3, width)
    params = lax.all_gather(params, ("h", "c"), axis=2, tiled=True)
    params = params.reshape(LAYERS, 3, blocks, LANES)

    def four(array, axes, both):
        pairs = [(i, i ^ 3) for i in range(4)]
        one = lax.ppermute(array, axes[1], FLIP2)
        two = lax.ppermute(array, axes[0], FLIP2)
        return [array, one, two, lax.ppermute(array, both, pairs)]

    def gather_stats(array):
        plane = jnp.stack(four(array, ("y", "x"), ("y", "x")))
        return four(plane, ("h", "c"), ("h", "c"))

    def far_share(layer):
        return lax.dynamic_slice(weights, (layer, b * rows, 0), (1, rows, depth))[0]

    near = swap(weights, 1)
    pieces = pack(place, inputs, frames)
    turned = pack(place, grad_out, frames)
    share = lax.ppermute(far_share(0), "h", FLIP2)
    own = [pieces[0], swap(pieces[1], 1)]
    others = [swap_half(piece) for piece in own]
    share, far_pieces = lax.optimization_barrier((share, (pieces[2:], params, turned)))
    own += [swap(piece, 2 + i) for i, piece in enumerate(far_pieces[0])]
    others += [swap_half(piece) for piece in own[2:]]
    far = assemble(y_x, *plane_gather(share))
    half_weights = [[weights, near, far, swap(far, 1)]]
    share = lax.ppermute(after(far_share(1), own), "h", FLIP2)
    far = lax.all_gather(share, ("y", "x"), axis=0, tiled=True)

    upstream = None
    saved = []
    chunk_plan = (2, 1)
    for layer in range(LAYERS):
        flat = layer == 0
        if layer > 0:
            others = [swap_half(piece) for piece in own]
            half_weights.append([weights, near, far, swap(after(far, z), 1)])
        other = others
        z, *own_flat = project(
            own_blocks, place, own, half_weights[layer], layer, flat=flat
        )
        z, stats, *other_flat = project(
            other_blocks, place, other, half_weights[layer], layer, z, valid, flat=flat
        )
        if layer == LAYERS - 1:
            turned = after(turned, z)
            upstream = [swap(piece, rel) for rel, piece in enumerate(turned)]
        stats = gather_stats(stats)
        chunks = chunk_plan[layer]
        pieces = 4 if layer == LAYERS - 1 else 1
        state = jnp.zeros((blocks, LANES), F32)
        following, states, slopes = [], [], []
        for chunk in range(chunks):
            *new, kept, slope, state = recur(
                chunk, chunks, place, gate, z, stats, params[layer], valid, state, own, pieces
            )
            following.extend(new)
            states.append(kept)
            slopes.append(slope)
        groups = [own_flat, other_flat] if flat else [own, other]
        groups = groups + [[swap(after(p, z), 1) for p in group] for group in groups]
        saved.append((groups, z, stats, states, slopes))
        own = following
    output = [swap(piece, rel) for rel, piece in enumerate(own)]

    ups = upstream
    results = [None] * LAYERS
    waiting = None
    axes = (("x", "y"), ("y", "x"))

    def second_step(halves):
        return [(t[0], lax.ppermute(t[1], axes[i][1], FLIP2)) for i, t in enumerate(halves)]

    def third_step(halves):
        totals = [kept + come for kept, come in halves]
        return [(t[0], lax.ppermute(t[1], "h", FLIP2)) for t in totals]

    for layer in range(LAYERS - 1, -1, -1):
        groups, z, stats, states, slopes = saved[layer]
        weight = half_weights[layer]
        grad_pre, sums = back(place, gate, z, stats, params[layer], ups, states, slopes)
        sums = tree(four(sums, ("y", "x"), ("y", "x")))
        if waiting is not None:
            totals = [kept + after(come, sums) for kept, come in waiting]
            sums = after(sums, totals)
            waiting = second_step(totals)
        sums = four(sums, ("h", "c"), ("h", "c"))
        grad_z, near_terms, far_terms, sums = norm_back(
            other_columns, place, grad_pre, z, params[layer], valid, stats, sums, weight, layer
        )
        if layer > 0:
            received = [swap_half(near_terms), swap_half(far_terms)]
        else:
            received = [swap_half(far_terms)]
        if waiting is not None:
            waiting = [(kept, after(come, grad_z)) for kept, come in waiting]
            waiting = third_step(waiting)
        leaving = jnp.concatenate(
            [grad_z[:, width : 2 * width], grad_z[:, 3 * width :]], axis=1
        )
        *first, turned = weight_terms(0, lists, place, (grad_z, swap(leaving, 1)), groups)
        second = list(weight_terms(1, lists, place, (turned,), groups))
        first[1] = lax.ppermute(first[1], "x", FLIP2)
        second[1] = lax.ppermute(second[1], "y", FLIP2)
        if layer == 0:
            near_terms = after(near_terms, received, second[0])
            received = [swap_half(near_terms)] + received
        kept = own_terms(own_columns, place, after(grad_z, second[0]), ups, weight, layer)
        ups = [kept, *received]
        if waiting is not None:
            done = [a + after(come, kept) for a, come in waiting]
            later = lax.all_gather(
                jnp.concatenate(done, axis=1), ("y", "x"), axis=0, tiled=True
            )
        waiting = [first, second]
        results[layer] = lax.dynamic_index_in_dim(
            sums.reshape(3, 4, width), clip, axis=1, keepdims=False
        )

    def grad_piece(rel):
        other = received[rel // 2]
        at = (rel % 2) * width
        return kept[:, rel * width : (rel + 1) * width] + other[:, at : at + width]

    far = [grad_piece(2), grad_piece(3)]
    grad_in = [swap(piece, 2 + i) for i, piece in enumerate(far)]
    waiting = second_step([a + after(come, far) for a, come in waiting])
    close = [grad_piece(0), grad_piece(1)]
    close = after(close, [come for _, come in waiting])
    grad_in = [close[0], swap(close[1], 1)] + grad_in
    waiting = third_step(waiting)
    output = unpack(place, after(output, [come for _, come in waiting][0]))
    grad_weights = keep(after(later, output), 1)
    shares = [a + after(come, grad_weights) for a, come in waiting]
    grad_weights = assemble(y_x, *plane_gather(*shares), 0, grad_weights)
    sums = jnp.stack(results)
    return (
        output,
        unpack(place, grad_in),
        grad_weights,
        sums[:, 0],
        sums[:, 1],
        sums[:, 2],
        sums[:, 1],
    )


def gelu_slope(value):
    return (
        0.5 * (1.0 + jax.scipy.special.erf(value / ROOT_TWO))
        + value * jnp.exp(-0.5 * value * value) / ROOT_TWO_PI
    )


def recur_step(decay, state, inputs):
    drive_t, valid_t = inputs
    pre = drive_t + decay * state
    state = state + valid_t * (jax.nn.gelu(pre, approximate=False) - state)
    return (state, state)


def back_step(decay, carry, inputs):
    upstream_t, valid_t, pre_t = inputs
    total = upstream_t + carry
    grad_pre = total * valid_t * gelu_slope(pre_t)
    carry = total * (1.0 - valid_t) + grad_pre * decay
    return (carry, grad_pre)


def add_piece(weight, piece):
    return jnp.dot(weight, piece, precision=HIGH, preferred_element_type=jnp.float32)


def weight_columns(grad_pre_norm, piece):
    return jnp.einsum("jf,kf->jk", grad_pre_norm, piece, precision=HIGH)


def split_features(inputs, weights, gains, shifts, decays, biases, lengths, frame_mask, grad_out):
    width, slots = inputs.shape
    clips, frames_len = frame_mask.shape
    frames = jnp.arange(frames_len, dtype=jnp.int32)
    valid_grid = (
        (frames[None, :] < lengths[:, None]) & ((frame_mask == 1) | (frames[None, :] == 0))
    ).astype(jnp.float32)
    valid = valid_grid.reshape(-1)
    valid_row = valid[None, :]
    valid_time = jnp.broadcast_to(valid_grid.T[:, :, None], (frames_len, clips, width)).reshape(
        frames_len, clips * width
    )
    count_local = jnp.sum(valid)

    def to_time(array):
        return jnp.transpose(array.reshape(width, clips, frames_len), (2, 1, 0)).reshape(
            frames_len, clips * width
        )

    def from_time(array):
        return jnp.transpose(array.reshape(frames_len, clips, width), (2, 1, 0)).reshape(
            width, slots
        )

    layer_in = inputs
    saved = []
    for layer_no in range(LAYERS):
        weight = weights[layer_no]
        gathered = lax.all_gather(layer_in, "neuron", axis=0, tiled=True)
        pre_norm = add_piece(weight, gathered)
        first_sum, count = lax.psum((jnp.sum(valid_row * pre_norm, axis=1), count_local), "batch")
        mean = first_sum / count
        centered = pre_norm - mean[:, None]
        var = lax.psum(jnp.sum(valid_row * centered * centered, axis=1), "batch") / count
        inv_std = lax.rsqrt(var + EPS)
        zhat = (pre_norm - mean[:, None]) * inv_std[:, None]
        drive = gains[layer_no][:, None] * zhat + (shifts[layer_no] + biases[layer_no])[:, None]
        drive_time = to_time(drive)
        decay_wide = jnp.tile(decays[layer_no], clips)
        start_state = jnp.zeros((clips * width,), jnp.float32)
        _, states = lax.scan(
            partial(recur_step, decay_wide), start_state, (drive_time, valid_time), unroll=8
        )
        saved.append((gathered, zhat, inv_std, drive_time, states, count))
        layer_in = layer_in + valid_row * from_time(states)
    upstream = grad_out
    grad_parts = [None] * LAYERS
    for layer_no in range(LAYERS - 1, -1, -1):
        gathered, zhat, inv_std, drive_time, states, count = saved[layer_no]
        decay_wide = jnp.tile(decays[layer_no], clips)
        gain = gains[layer_no]
        previous = jnp.concatenate([jnp.zeros_like(states[:1]), states[:-1]], axis=0)
        pre_time = drive_time + decay_wide[None, :] * previous
        grad_state = to_time(valid_row * upstream)
        start_carry = jnp.zeros((clips * width,), jnp.float32)
        _, grad_pre_time = lax.scan(
            partial(back_step, decay_wide),
            start_carry,
            (grad_state, valid_time, pre_time),
            reverse=True,
            unroll=8,
        )
        decay_local = jnp.sum(
            jnp.sum(grad_pre_time * previous, axis=0).reshape(clips, width), axis=0
        )
        grad_pre = from_time(grad_pre_time)
        gain_local = jnp.sum(grad_pre * zhat, axis=1)
        shift_local = jnp.sum(grad_pre, axis=1)
        grad_gain, grad_shift, grad_decay = lax.psum(
            (gain_local, shift_local, decay_local), "batch"
        )
        grad_pre_norm = (gain * inv_std)[:, None] * (
            grad_pre - valid_row * (grad_shift[:, None] + zhat * grad_gain[:, None]) / count
        )
        weight_local = weight_columns(grad_pre_norm, gathered)
        input_terms = jnp.einsum("jk,jf->kf", weights[layer_no], grad_pre_norm, precision=HIGH)
        input_grad = lax.psum_scatter(input_terms, "neuron", scatter_dimension=0, tiled=True)
        grad_weight = lax.psum(weight_local, "batch")
        upstream = upstream + input_grad
        grad_parts[layer_no] = (grad_weight, grad_gain, grad_shift, grad_decay)
    grad_weights = jnp.stack([grad_parts[layer_no][0] for layer_no in range(LAYERS)])
    grad_gains = jnp.stack([grad_parts[layer_no][1] for layer_no in range(LAYERS)])
    grad_shifts = jnp.stack([grad_parts[layer_no][2] for layer_no in range(LAYERS)])
    grad_decays = jnp.stack([grad_parts[layer_no][3] for layer_no in range(LAYERS)])
    return (layer_in, upstream, grad_weights, grad_gains, grad_shifts, grad_decays, grad_shifts)


def solution(mesh):
    if (mesh.shape["batch"], mesh.shape["neuron"]) == (4, 8):
        cut = Mesh(mesh.devices.reshape(2, 2, 2, 2, 2), ("y", "x", "h", "l", "c"))
        batch, neuron, body = ("y", "x"), ("h", "l", "c"), half_features
    else:
        cut, batch, neuron, body = mesh, "batch", "neuron", split_features
    in_specs = (
        P(neuron, batch),
        P(None, neuron, None),
        P(None, neuron),
        P(None, neuron),
        P(None, neuron),
        P(None, neuron),
        P(batch),
        P(batch, None),
        P(neuron, batch),
    )
    out_specs = (
        P(neuron, batch),
        P(neuron, batch),
        P(None, neuron, None),
        P(None, neuron),
        P(None, neuron),
        P(None, neuron),
        P(None, neuron),
    )
    return jax.shard_map(
        body, mesh=cut, in_specs=in_specs, out_specs=out_specs, check_vma=False
    )
```

```python
from functools import partial
import math

import jax
import jax.numpy as jnp
from jax import lax
from jax.experimental import pallas as pl
from jax.experimental.pallas import tpu as pltpu
from jax.sharding import Mesh, PartitionSpec as P

LAYERS = 2
EPS = 1e-05
HIGH = lax.Precision.HIGHEST
ROOT_TWO = math.sqrt(2.0)
ROOT_TWO_PI = math.sqrt(2.0 * math.pi)
F32 = jnp.float32
BF16 = jnp.bfloat16
LANES = 128
VMEM_LIMIT = 48 * 1024 * 1024
SMEM_SPEC = pl.BlockSpec(memory_space=pltpu.SMEM)
VMEM_SPEC = pl.BlockSpec(memory_space=pltpu.VMEM)


FLIP2 = [(0, 1), (1, 0)]


def flip_of(rel):
    if rel == 1:
        return "c", FLIP2
    if rel == 2:
        return "h", FLIP2
    return ("h", "c"), [(i, i ^ 3) for i in range(4)]


def swap(array, rel):
    if rel == 0:
        return array
    axes, pairs = flip_of(rel)
    return lax.ppermute(array, axes, pairs)


def swap_half(array):
    return lax.ppermute(array, "l", FLIP2)


def split(value):
    high = value.astype(BF16)
    return high, (value - high.astype(F32)).astype(BF16)


def dot(a, b, dims):
    return lax.dot_general(a, b, (dims, ((), ())), preferred_element_type=F32)


NT = ((1,), (1,))
NN = ((1,), (0,))


def call(body, **kwargs):
    return pl.pallas_call(
        body,
        compiler_params=pltpu.CompilerParams(vmem_limit_bytes=VMEM_LIMIT),
        **kwargs,
    )


def cost(flops, byte_count):
    return pl.CostEstimate(flops=int(flops) // 64, bytes_accessed=int(byte_count) // 64, transcendentals=0)


def pack_body(frames, place_ref, in_ref, *refs):
    outs, turned = refs[:4], refs[4]
    slots = in_ref.shape[1]
    for start in range(0, slots, LANES):
        turned[start : start + LANES, :] = in_ref[:, start : start + LANES].T
    for rel in range(4):
        first = pl.multiple_of(place_ref[rel] * frames, 8)
        outs[rel][...] = turned[pl.ds(first, frames), :]


def pack(place, array, frames):
    width, slots = array.shape
    return call(
        partial(pack_body, frames),
        out_shape=[jax.ShapeDtypeStruct((frames, width), F32)] * 4,
        in_specs=[SMEM_SPEC, VMEM_SPEC],
        out_specs=[VMEM_SPEC] * 4,
        scratch_shapes=[pltpu.VMEM((slots, width), F32)],
        cost_estimate=cost(0, 8 * width * slots),
        name="pack",
    )(place, array)


def unpack_body(frames, place_ref, *refs):
    ins, out_ref, turned = refs[:4], refs[4], refs[5]
    slots = out_ref.shape[1]
    for rel in range(4):
        first = pl.multiple_of(place_ref[rel] * frames, 8)
        turned[pl.ds(first, frames), :] = ins[rel][...]
    for start in range(0, slots, LANES):
        out_ref[:, start : start + LANES] = turned[start : start + LANES, :].T


def unpack(place, pieces):
    frames, width = pieces[0].shape
    slots = 4 * frames
    return call(
        partial(unpack_body, frames),
        out_shape=jax.ShapeDtypeStruct((width, slots), F32),
        in_specs=[SMEM_SPEC] + [VMEM_SPEC] * 4,
        out_specs=VMEM_SPEC,
        scratch_shapes=[pltpu.VMEM((slots, width), F32)],
        cost_estimate=cost(0, 8 * width * slots),
        name="unpack",
    )(place, *pieces)


def spread_of(parts, width):
    spots, row, column = [], 0, 0
    for part in parts:
        spots.append((row, column))
        if part.shape[1] == width:
            column += width
        else:
            row += part.shape[0]
    return spots


def project_body(n_parts, spots, with_acc, with_stats, flat, cols_ref, place_ref, *refs):
    del cols_ref
    parts, refs = refs[:n_parts], refs[n_parts:]
    weights, refs = refs[:4], refs[4:]
    if with_acc:
        acc_ref, refs = refs[0], refs[1:]
    if with_stats:
        valid_ref, refs = refs[0], refs[1:]
    out_ref, refs = refs[0], refs[1:]
    if with_stats:
        stats_ref, refs = refs[0], refs[1:]
    if flat:
        flat_ref, refs = refs[0], refs[1:]
    x_high, x_low = refs
    step = pl.program_id(0)
    width = x_high.shape[2]

    @pl.when(step == 0)
    def _():
        for (row, column), part in zip(spots, parts):
            rows, columns = part.shape
            for start in range(0, columns, width):
                rel = (column + start) // width
                high, low = split(part[:, start : start + width])
                x_high[rel, row : row + rows, :] = high
                x_low[rel, row : row + rows, :] = low
            if flat:
                flat_ref[row : row + rows, column : column + columns] = part[...]
        if with_acc:
            out_ref[...] = acc_ref[...]
        else:
            out_ref[...] = jnp.zeros_like(out_ref)

    stacked = jnp.concatenate([x_high[step], x_low[step], x_high[step]], axis=1)
    for block in range(4):
        w_high, w_low = split(weights[block][...].reshape(width, width))
        columns = slice(block * width, (block + 1) * width)
        out_ref[:, columns] += dot(stacked, jnp.concatenate([w_high, w_high, w_low], axis=1), NT)

    if with_stats:

        @pl.when(step == pl.num_programs(0) - 1)
        def _():
            valid = valid_ref[...]
            own = jnp.sum(valid, axis=0, keepdims=True)
            per = width // LANES
            for row in range(out_ref.shape[1] // LANES):
                z = out_ref[:, row * LANES : (row + 1) * LANES]
                total = jnp.sum(valid * z, axis=0, keepdims=True)
                centred = valid * (z - total / own)
                squares = jnp.sum(centred * centred, axis=0, keepdims=True)
                at = place_ref[row // per] * per + row % per
                stats_ref[0, pl.ds(at, 1), :] = total
                stats_ref[1, pl.ds(at, 1), :] = squares
                stats_ref[2, pl.ds(at, 1), :] = own


def weight_specs(weights, layer, pairs=2):
    specs = []
    for weight in weights:
        width = weight.shape[-2]
        if weight.ndim == 3:
            specs.append(
                pl.BlockSpec((1, width, pairs * width), lambda s, cols, *_: (layer, 0, cols[s]))
            )
        else:
            specs.append(pl.BlockSpec((width, pairs * width), lambda s, cols, *_: (0, cols[s])))
    return specs


def project(columns, place, parts, weights, layer, acc=None, valid=None, flat=False):
    width = weights[0].shape[-2]
    frames = sum(p.shape[0] for p in parts if p.shape[1] != width) or parts[0].shape[0]
    full = pl.BlockSpec(memory_space=pltpu.VMEM)
    in_specs = [full] * len(parts)
    in_specs += weight_specs(weights, layer, 1)
    operands = list(parts) + list(weights)
    array = jax.ShapeDtypeStruct((frames, 4 * width), F32)
    array_spec = pl.BlockSpec((frames, 4 * width), lambda s, cols, place: (0, 0))
    out_shape, out_specs = [array], [array_spec]
    if acc is not None:
        in_specs.append(full)
        operands.append(acc)
    if valid is not None:
        in_specs.append(full)
        operands.append(valid)
        rows = 4 * width // LANES
        out_shape.append(jax.ShapeDtypeStruct((3, rows, LANES), F32))
        out_specs.append(pl.BlockSpec((3, rows, LANES), lambda s, cols, place: (0, 0, 0)))
    if flat:
        out_shape.append(array)
        out_specs.append(array_spec)
    return call(
        partial(
            project_body,
            len(parts),
            spread_of(parts, width),
            acc is not None,
            valid is not None,
            flat,
        ),
        grid_spec=pltpu.PrefetchScalarGridSpec(
            num_scalar_prefetch=2,
            grid=(4,),
            in_specs=in_specs,
            out_specs=out_specs,
            scratch_shapes=[pltpu.VMEM((4, frames, width), BF16)] * 2,
        ),
        out_shape=out_shape,
        cost_estimate=cost(2 * 3 * frames * 16 * width * width, 4 * 16 * width * width),
        name="project",
    )(columns, place, *operands)


def to_relative(place_ref, spread, rows_ref, value, slot):
    per = value.shape[0] // 4
    spread[...] = value
    for rel in range(4):
        first = place_ref[rel] * per
        for row in range(per):
            rows_ref[slot, rel * per + row : rel * per + row + 1, :] = spread[
                pl.ds(first + row, 1), :
            ]


def tree(values):
    while len(values) > 1:
        values = [a + b for a, b in zip(values[::2], values[1::2])]
    return values[0]


def norm_terms(stats_ref):
    each = [[stats_ref[i, slot] for i in range(stats_ref.shape[0])] for slot in range(3)]
    totals, squares, owns = each
    count = tree(owns)
    mean = tree(totals) / count
    away = [total / own - mean for total, own in zip(totals, owns)]
    spread = tree([s + n * a * a for s, n, a in zip(squares, owns, away)])
    return count, mean, lax.rsqrt(spread / count + EPS)


def recur_body(n_parts, spots, out_cols, first, place_ref, gate_ref, z_ref, stats_ref, params_ref, valid_ref, start_ref, *refs):
    parts, refs = refs[:n_parts], refs[n_parts:]
    n_out = len(out_cols)
    outs, refs = refs[:n_out], refs[n_out:]
    state_ref, slope_ref, last_ref, rows, spread, drive_s, state_s, slope_s = refs
    frames = z_ref.shape[0]
    blocks = z_ref.shape[1] // LANES
    _, mean, inv_std = norm_terms(stats_ref)
    to_relative(place_ref, spread, rows, mean, 0)
    to_relative(place_ref, spread, rows, params_ref[0] * inv_std, 1)
    to_relative(place_ref, spread, rows, params_ref[1], 2)
    to_relative(place_ref, spread, rows, params_ref[2], 3)
    for row in range(blocks):
        z = z_ref[:, row * LANES : (row + 1) * LANES]
        drive_s[row * frames : (row + 1) * frames, :] = (
            z - rows[0, row : row + 1, :]
        ) * rows[1, row : row + 1, :] + rows[2, row : row + 1, :]
    decay = rows[3]

    def step(t, state):
        at = pl.ds(t, blocks, stride=frames)
        pre = drive_s[at, :] + decay * state
        half = 0.5 + 0.5 * lax.erf(pre * (1.0 / ROOT_TWO))
        gate = gate_ref[first + t] > 0.0
        slope = half + pre * jnp.exp(-0.5 * pre * pre) * (1.0 / ROOT_TWO_PI)
        state = jnp.where(gate, pre * half, state)
        state_s[at, :] = state
        slope_s[at, :] = jnp.where(gate, slope, 0.0)
        return state

    last_ref[...] = lax.fori_loop(0, frames, step, start_ref[...], unroll=8)
    valid = valid_ref[...]
    for row in range(blocks):
        lanes = slice(row * LANES, (row + 1) * LANES)
        state = state_s[row * frames : (row + 1) * frames, :]
        state_ref[:, lanes] = state
        slope_ref[:, lanes] = slope_s[row * frames : (row + 1) * frames, :]
        for (top, column), part in zip(spots, parts):
            if column <= row * LANES < column + part.shape[1]:
                x = part[:, row * LANES - column : (row + 1) * LANES - column]
                some = slice(top, top + part.shape[0])
                for out_column, out in zip(out_cols, outs):
                    if out_column <= row * LANES < out_column + out.shape[1]:
                        at = row * LANES - out_column
                        out[some, at : at + LANES] = x + valid[some] * state[some]


def recur(chunk, chunks, place, gate, z, stats, params, valid, start, parts, pieces):
    frames = z.shape[0] // chunks
    features = z.shape[1]
    width = features // 4
    blocks = features // LANES
    row_block = lambda columns: pl.BlockSpec((frames, columns), lambda i: (chunk, 0))
    whole = lambda array: pl.BlockSpec(array.shape, lambda i: (0,) * array.ndim)
    part_specs = [row_block(p.shape[1]) if p.shape[0] == z.shape[0] else whole(p) for p in parts]
    n_out = pieces
    out_width = features // n_out
    tile = jax.ShapeDtypeStruct((blocks, LANES), F32)
    full = jax.ShapeDtypeStruct((frames, features), F32)
    out_shape = [jax.ShapeDtypeStruct((frames, out_width), F32)] * n_out + [full, full, tile]
    return call(
        partial(
            recur_body,
            len(parts),
            spread_of(parts, width),
            [i * out_width for i in range(n_out)],
            chunk * frames,
        ),
        grid=(1,),
        in_specs=[
            SMEM_SPEC,
            SMEM_SPEC,
            row_block(features),
            whole(stats),
            whole(params),
            row_block(LANES),
            whole(start),
        ]
        + part_specs,
        out_specs=[whole(s) for s in out_shape],
        out_shape=out_shape,
        scratch_shapes=[
            pltpu.VMEM((4, blocks, LANES), F32),
            pltpu.VMEM((blocks, LANES), F32),
        ]
        + [pltpu.VMEM((blocks * frames, LANES), F32)] * 3,
        cost_estimate=cost(100 * frames * features, 20 * frames * features),
        name="recur",
    )(place, gate, z, stats, params, valid, start, *parts)


def back_body(n_parts, spots, n_state, place_ref, gate_ref, z_ref, stats_ref, params_ref, *refs):
    parts, refs = refs[:n_parts], refs[n_parts:]
    states, refs = refs[:n_state], refs[n_state:]
    slopes, refs = refs[:n_state], refs[n_state:]
    grad_ref, sums_ref, rows, spread, up_s, state_s, slope_s = refs
    frames = z_ref.shape[0]
    blocks = z_ref.shape[1] // LANES
    tall = frames + 8
    _, mean, inv_std = norm_terms(stats_ref)
    to_relative(place_ref, spread, rows, mean, 0)
    to_relative(place_ref, spread, rows, inv_std, 1)
    to_relative(place_ref, spread, rows, params_ref[2], 2)
    for row in range(blocks):
        lanes = slice(row * LANES, (row + 1) * LANES)
        base = row * frames
        up = None
        for (top, column), part in zip(spots, parts):
            if column <= row * LANES < column + part.shape[1] and part.shape[0] == frames:
                value = part[:, row * LANES - column : (row + 1) * LANES - column]
                up = value if up is None else up + value
        up_s[base : base + frames, :] = up
        state_s[row * tall : row * tall + 8, :] = jnp.zeros((8, LANES), F32)
        first = 0
        for state, slope in zip(states, slopes):
            some = state.shape[0]
            at = row * tall + 8 + first
            state_s[at : at + some, :] = state[:, lanes]
            slope_s[base + first : base + first + some, :] = slope[:, lanes]
            first += some
    decay = rows[2]

    def step(i, carry):
        t = frames - 1 - i
        at = pl.ds(t, blocks, stride=frames)
        slope = slope_s[at, :]
        gate = gate_ref[t]
        total = gate * up_s[at, :] + carry
        up_s[at, :] = total * slope
        return total * (slope * decay + (1.0 - gate))

    lax.fori_loop(0, frames, step, jnp.zeros((blocks, LANES), F32), unroll=8)
    per = blocks // 4
    for row in range(blocks):
        lanes = slice(row * LANES, (row + 1) * LANES)
        base = row * frames
        grad = up_s[base : base + frames, :]
        grad_ref[:, lanes] = grad
        zhat = (z_ref[:, lanes] - rows[0, row : row + 1, :]) * rows[1, row : row + 1, :]
        before = state_s[row * tall + 7 : row * tall + 7 + frames, :]
        at = place_ref[row // per] * per + row % per
        for slot, value in enumerate((grad * zhat, grad, grad * before)):
            sums_ref[slot, pl.ds(at, 1), :] = jnp.sum(value, axis=0, keepdims=True)


def spots_of_sum(parts, width):
    spots, column = [], 0
    for part in parts:
        spots.append((0, column % (4 * width)))
        column += part.shape[1]
    return spots


def back(place, gate, z, stats, params, ups, states, slopes):
    frames, features = z.shape
    width = features // 4
    blocks = features // LANES
    return call(
        partial(back_body, len(ups), spots_of_sum(ups, width), len(states)),
        in_specs=[SMEM_SPEC] * 2 + [VMEM_SPEC] * (3 + len(ups) + 2 * len(states)),
        out_specs=[VMEM_SPEC] * 2,
        out_shape=[
            jax.ShapeDtypeStruct((frames, features), F32),
            jax.ShapeDtypeStruct((3, blocks, LANES), F32),
        ],
        scratch_shapes=[
            pltpu.VMEM((3, blocks, LANES), F32),
            pltpu.VMEM((blocks, LANES), F32),
            pltpu.VMEM((blocks * frames, LANES), F32),
            pltpu.VMEM((blocks * (frames + 8), LANES), F32),
            pltpu.VMEM((blocks * frames, LANES), F32),
        ],
        cost_estimate=cost(30 * frames * features, 20 * frames * features),
        name="back",
    )(place, gate, z, stats, params, *ups, *states, *slopes)


def input_terms(high_s, low_s, weights):
    width = high_s.shape[2]
    left, right = [], []
    for block, weight in enumerate(weights):
        w_high, w_low = split(weight[...].reshape(width, 2 * width))
        left += [high_s[block], low_s[block], high_s[block]]
        right += [w_high, w_high, w_low]
    return dot(jnp.concatenate(left, axis=1), jnp.concatenate(right, axis=0), NN)


def norm_back_body(cols_ref, place_ref, grad_ref, z_ref, params_ref, valid_ref, stats_ref, sums_ref, *refs):
    del cols_ref
    weights, refs = refs[:4], refs[4:]
    out_ref, leave_ref, near_term_ref, far_term_ref, sums_out_ref, rows, spread, high_s, low_s = refs
    blocks = z_ref.shape[1] // LANES
    width = high_s.shape[2]
    per = width // LANES

    @pl.when(pl.program_id(0) == 0)
    def _():
        count, mean, inv_std = norm_terms(stats_ref)
        to_relative(place_ref, spread, rows, mean, 0)
        to_relative(place_ref, spread, rows, inv_std, 1)
        to_relative(place_ref, spread, rows, params_ref[0] * inv_std, 2)
        sums = tree([sums_ref[i] for i in range(sums_ref.shape[0])])
        sums_out_ref[...] = sums
        to_relative(place_ref, spread, rows, sums[0] / count, 3)
        to_relative(place_ref, spread, rows, sums[1] / count, 4)
        valid = valid_ref[...]
        for row in range(blocks):
            lanes = slice(row * LANES, (row + 1) * LANES)
            one = lambda slot: rows[slot, row : row + 1, :]
            zhat = (z_ref[:, lanes] - one(0)) * one(1)
            value = one(2) * (grad_ref[:, lanes] - valid * (one(4) + zhat * one(3)))
            out_ref[:, lanes] = value
            if (row // per) % 2:
                at = (row // per // 2) * width + (row % per) * LANES
                leave_ref[:, at : at + LANES] = value
            high, low = split(value)
            inner = slice((row % per) * LANES, (row % per + 1) * LANES)
            high_s[row // per, :, inner] = high
            low_s[row // per, :, inner] = low

    value = input_terms(high_s, low_s, weights)
    for step, term_ref in enumerate((far_term_ref, near_term_ref)):

        @pl.when(pl.program_id(0) == step)
        def _():
            for pair in range(2):
                at = pl.multiple_of(((place_ref[0] & 1) ^ pair) * width, width)
                term_ref[:, pl.ds(at, width)] = value[:, pair * width : (pair + 1) * width]


def norm_back(columns, place, grad, z, params, valid, stats, sums, weights, layer):
    frames, features = z.shape
    width = features // 4
    blocks = features // LANES
    whole = lambda array: pl.BlockSpec(array.shape, lambda s, cols, place: (0,) * array.ndim)
    operands = [grad, z, params, valid, stats, sums]
    full = jax.ShapeDtypeStruct((frames, features), F32)
    half = jax.ShapeDtypeStruct((frames, 2 * width), F32)
    out_shape = [full, half, half, half, jax.ShapeDtypeStruct((3, blocks, LANES), F32)]
    return call(
        norm_back_body,
        grid_spec=pltpu.PrefetchScalarGridSpec(
            num_scalar_prefetch=2,
            grid=(2,),
            in_specs=[whole(a) for a in operands] + weight_specs(weights, layer),
            out_specs=[whole(a) for a in out_shape],
            scratch_shapes=[
                pltpu.VMEM((5, blocks, LANES), F32),
                pltpu.VMEM((blocks, LANES), F32),
                pltpu.VMEM((4, frames, width), BF16),
                pltpu.VMEM((4, frames, width), BF16),
            ],
        ),
        out_shape=out_shape,
        cost_estimate=cost(6 * frames * features * features, 4 * features * features),
        name="norm_back",
    )(columns, place, *operands, *weights)


def own_terms_body(n_ups, spots, cols_ref, place_ref, grad_ref, *refs):
    del cols_ref
    ups, refs = refs[:n_ups], refs[n_ups:]
    weights, refs = refs[:4], refs[4:]
    out_ref, high_s, low_s = refs
    width = high_s.shape[2]
    step = pl.program_id(0)

    @pl.when(step == 0)
    def _():
        for block in range(4):
            high, low = split(grad_ref[:, block * width : (block + 1) * width])
            high_s[block] = high
            low_s[block] = low

    value = input_terms(high_s, low_s, weights)
    for pair in range(2):
        at = pl.multiple_of(((place_ref[0] & 1) ^ pair) * width, width)
        out_ref[:, pl.ds(at, width)] = value[:, pair * width : (pair + 1) * width]
    for half in range(2):

        @pl.when(step == half)
        def _():
            first = 2 * half * width
            for (_, column), up in zip(spots, ups):
                low = max(column, first)
                high = min(column + up.shape[1], first + 2 * width)
                if low < high:
                    out_ref[:, low - first : high - first] += up[:, low - column : high - column]


def own_terms(columns, place, grad, ups, weights, layer):
    frames, features = grad.shape
    width = features // 4
    whole = lambda array: pl.BlockSpec(array.shape, lambda s, cols, place: (0,) * array.ndim)
    step_block = pl.BlockSpec((frames, 2 * width), lambda s, cols, place: (0, s))
    return call(
        partial(own_terms_body, len(ups), spots_of_sum(ups, width)),
        grid_spec=pltpu.PrefetchScalarGridSpec(
            num_scalar_prefetch=2,
            grid=(2,),
            in_specs=[whole(a) for a in (grad, *ups)]
            + weight_specs(weights, layer),
            out_specs=step_block,
            scratch_shapes=[pltpu.VMEM((4, frames, width), BF16)] * 2,
        ),
        out_shape=jax.ShapeDtypeStruct((frames, features), F32),
        cost_estimate=cost(6 * frames * features * features, 4 * features * features),
        name="own_terms",
    )(columns, place, grad, *ups, *weights)


def prepare_body(n_chunks, lists_ref, *refs):
    del lists_ref
    groups = []
    for _ in range(4):
        groups.append(refs[:n_chunks])
        refs = refs[n_chunks:]
    high_ref, low_ref = refs
    padded = high_ref.shape[0] // 2
    for side in range(2):

        @pl.when(pl.program_id(0) // 4 == side)
        def _():
            for clip in range(2):
                row = clip * padded
                for part in groups[2 * clip + side]:
                    rows = part.shape[0]
                    high, low = split(part[...])
                    high_ref[row : row + rows, :] = high
                    low_ref[row : row + rows, :] = low
                    row += rows
                rest = (clip + 1) * padded - row
                zeros = jnp.zeros((rest, high_ref.shape[1]), BF16)
                high_ref[row : row + rest, :] = zeros
                low_ref[row : row + rest, :] = zeros


def prepare(lists, groups):
    width = groups[0][0].shape[1] // 4
    frames = sum(part.shape[0] for part in groups[0])
    padded = -(-frames // LANES) * LANES
    in_specs = []
    for i, group in enumerate(groups):
        for part in group:
            if i % 2 == 0:
                index = lambda s, cols, flip=i // 2: (0, jnp.minimum(s, 3) ^ flip)
            else:
                index = lambda s, cols, flip=i // 2: (0, jnp.maximum(s - 4, 0) ^ flip)
            in_specs.append(pl.BlockSpec((part.shape[0], width), index))
    out = jax.ShapeDtypeStruct((2 * padded, 8 * width), BF16)
    return call(
        partial(prepare_body, len(groups[0])),
        grid_spec=pltpu.PrefetchScalarGridSpec(
            num_scalar_prefetch=1,
            grid=(8,),
            in_specs=in_specs,
            out_specs=[pl.BlockSpec((2 * padded, width), lambda s, cols: (0, cols[s]))] * 2,
        ),
        out_shape=[out, out],
        cost_estimate=cost(0, 16 * frames * 8 * width),
        name="prepare",
    )(lists, *[part for group in groups for part in group])


def product(g_high, g_low, x_high, x_low):
    return dot(g_high, x_high, NN) + (dot(g_high, x_low, NN) + dot(g_low, x_high, NN))


def leaving_body(turn, place_ref, *refs):
    if turn:
        grad_ref, near_ref, x_high, x_low, sent, g_high, g_low, t_high, t_low = refs

        @pl.when(pl.program_id(0) == 0)
        def _():
            frames, features = grad_ref.shape
            width = features // 4
            rows = width // 4
            padded = t_high.shape[1] // 2
            t_high[...] = jnp.zeros_like(t_high)
            t_low[...] = jnp.zeros_like(t_low)
            for clip in range(2):
                for dh in range(2):
                    if clip == 0:
                        part = grad_ref[:, 2 * dh * width : (2 * dh + 1) * width]
                    else:
                        part = near_ref[:, dh * width : (dh + 1) * width]
                    high, low = split(part.T)
                    at = (slice(dh * width, (dh + 1) * width), slice(clip * padded, clip * padded + frames))
                    t_high[at] = high
                    t_low[at] = low
            for group in range(8):
                first, second, dh = group // 4, group // 2 % 2, group % 2
                core = place_ref[6]
                y = place_ref[4] ^ (first * core + second * (1 - core))
                x = place_ref[5] ^ (first * (1 - core) + second * core)
                at = pl.multiple_of(dh * width + (2 * y + x) * rows, rows)
                g_high[group * rows : (group + 1) * rows, :] = t_high[pl.ds(at, rows), :]
                g_low[group * rows : (group + 1) * rows, :] = t_low[pl.ds(at, rows), :]

    else:
        g_high, g_low, x_high, x_low, sent = refs
    half = g_high.shape[0] // 2
    value = product(g_high[half:, :], g_low[half:, :], x_high[...], x_low[...])
    sent[...] = value.reshape(sent.shape)


def leaving_rows(half, place, grads, x_split, width):
    turn = half == 0
    whole = lambda array: pl.BlockSpec(array.shape, lambda s, place: (0,) * array.ndim)
    x_spec = pl.BlockSpec((x_split[0].shape[0], width), lambda s, place: (0, 4 * half + s))
    shape = (2, 2, width // 4, 4 * width)
    out_shape = [jax.ShapeDtypeStruct(shape, F32)]
    out_specs = [pl.BlockSpec(shape[:3] + (width,), lambda s, place: (0, 0, 0, s))]
    scratch = []
    if turn:
        turned = (2 * width, x_split[0].shape[0])
        out_shape += [jax.ShapeDtypeStruct(turned, BF16)] * 2
        out_specs += [whole(out_shape[-1])] * 2
        scratch = [pltpu.VMEM(turned, BF16)] * 2
    return call(
        partial(leaving_body, turn),
        grid_spec=pltpu.PrefetchScalarGridSpec(
            num_scalar_prefetch=1,
            grid=(4,),
            in_specs=[whole(a) for a in grads] + [x_spec] * 2,
            out_specs=out_specs,
            scratch_shapes=scratch,
        ),
        out_shape=out_shape,
        cost_estimate=cost(6 * x_split[0].shape[0] * width * 4 * width, 4 * 4 * width * width),
        name="leaving_rows",
    )(place, *grads, *x_split)


def staying_body(g_high, g_low, x_high, x_low, kept):
    half = g_high.shape[0] // 2
    value = product(g_high[:half, :], g_low[:half, :], x_high[...], x_low[...])
    kept[...] = value.reshape(kept.shape)


def staying_rows(turned, x_split, width):
    whole = lambda array: pl.BlockSpec(array.shape, lambda s: (0,) * array.ndim)
    x_spec = pl.BlockSpec((x_split[0].shape[0], width), lambda s: (0, s))
    shape = (2, 2, width // 4, 8 * width)
    return call(
        staying_body,
        grid=(8,),
        in_specs=[whole(a) for a in turned] + [x_spec] * 2,
        out_specs=pl.BlockSpec(shape[:3] + (width,), lambda s: (0, 0, 0, s)),
        out_shape=jax.ShapeDtypeStruct(shape, F32),
        cost_estimate=cost(6 * x_split[0].shape[0] * width * 8 * width, 4 * 8 * width * width),
        name="staying_rows",
    )(*turned, *x_split)


def plane_swap(array, step):
    pairs = []
    for i in range(8):
        over_x = (i % 2 == 0) == (step == 0)
        pairs.append((i, i ^ 2 if over_x else i ^ 4))
    return lax.ppermute(array, ("y", "x", "c"), pairs)


def plane_gather(share):
    first = plane_swap(share, 0)
    second = plane_swap(share, 1)
    return [share, second, first, plane_swap(first, 1)]


def assemble_body(groups, place_ref, *refs):
    out_ref = refs[-1]
    core = place_ref[6]
    column = 0
    for group in range(groups):
        rows, columns = refs[4 * group].shape
        for i in range(4):
            first, second = i // 2, i % 2
            y = place_ref[4] ^ (first * core + second * (1 - core))
            x = place_ref[5] ^ (first * (1 - core) + second * core)
            at = pl.multiple_of((2 * y + x) * rows, rows)
            out_ref[..., pl.ds(at, rows), column : column + columns] = refs[4 * group + i][
                ...
            ].reshape(out_ref.shape[:-2] + (rows, columns))
        column += columns


def assemble(place, groups, layer=None, onto=None):
    pieces = [piece for group in groups for piece in group]
    rows = pieces[0].shape[0]
    shape = (4 * rows, sum(group[0].shape[1] for group in groups))
    out_spec = pl.BlockSpec(shape, lambda i: (0, 0))
    aliases, extra, extra_specs = {}, [], []
    if layer is not None:
        out_spec = pl.BlockSpec((1, *shape), lambda i: (layer, 0, 0))
        aliases, extra = {1 + len(pieces): 0}, [onto]
        extra_specs = [pl.BlockSpec(memory_space=pl.ANY)]
        shape = (LAYERS, *shape)
    return call(
        partial(assemble_body, len(groups)),
        grid=(1,),
        out_shape=jax.ShapeDtypeStruct(shape, F32),
        in_specs=[SMEM_SPEC]
        + [pl.BlockSpec(p.shape, lambda i: (0, 0)) for p in pieces]
        + extra_specs,
        out_specs=out_spec,
        input_output_aliases=aliases,
        cost_estimate=cost(0, 8 * shape[-1] * shape[-2]),
        name="assemble",
    )(place, *pieces, *extra)


def keep_body(in_ref, out_ref):
    out_ref[0] = in_ref[...]


def keep(array, layer):
    return call(
        keep_body,
        grid=(1,),
        out_shape=jax.ShapeDtypeStruct((LAYERS, *array.shape), F32),
        in_specs=[pl.BlockSpec(array.shape, lambda i: (0, 0))],
        out_specs=pl.BlockSpec((1, *array.shape), lambda i: (layer, 0, 0)),
        cost_estimate=cost(0, 8 * array.size),
        name="keep",
    )(array)


def after(value, *others):
    return lax.optimization_barrier((value, others))[0]


def half_features(inputs, weights, gains, shifts, decays, biases, lengths, frame_mask, grad_out):
    width, slots = inputs.shape
    clips, frames = frame_mask.shape
    depth = weights.shape[2]
    blocks = 4 * width // LANES
    y, x, h, l, c = (lax.axis_index(name) for name in ("y", "x", "h", "l", "c"))
    b = 2 * y + x
    numbers = [2 * (h ^ (rel // 2)) + (c ^ (rel % 2)) for rel in range(4)] + [y, x, c]
    place = jnp.stack(numbers).astype(jnp.int32)
    own_blocks, other_blocks = (
        jnp.stack(
            [2 * (2 * (h ^ (rel // 2)) + half) + (c ^ (rel % 2)) for rel in range(4)]
        ).astype(jnp.int32)
        for half in (l, 1 - l)
    )
    all_blocks = jnp.concatenate([own_blocks, other_blocks])
    own_columns = jnp.stack([2 * h + l, 2 * (1 - h) + l]).astype(jnp.int32)
    other_columns = jnp.stack([2 * (1 - h) + 1 - l, 2 * h + 1 - l]).astype(jnp.int32)
    rows = width // 4

    clip = 2 * h + c
    seen = lax.dynamic_index_in_dim(frame_mask, clip, 0, keepdims=False)
    length = lax.dynamic_index_in_dim(lengths, clip, 0, keepdims=False)
    moments = jnp.arange(frames, dtype=jnp.int32)
    gate = ((moments < length) & ((seen == 1) | (moments == 0))).astype(F32)
    valid = jnp.broadcast_to(gate[:, None], (frames, LANES))

    def gather_sums(array, between=lambda stage: stage):
        plane = between(lax.all_gather(array, ("y", "x")))
        return lax.all_gather(plane, ("h", "c")).reshape(16, *array.shape)

    def far_share(layer):
        return lax.dynamic_slice(weights, (layer, b * rows, 0), (1, rows, depth))[0]

    near = swap(weights, 1)
    share = far_share(0)
    pieces = pack(place, after(inputs, share), frames)
    share = lax.ppermute(share, "h", FLIP2)
    own = [pieces[0], swap(pieces[1], 1)]
    others = [swap_half(piece) for piece in own]
    turned = pack(place, after(grad_out, pieces), frames)
    params = jnp.stack([gains, shifts + biases, decays], axis=1).reshape(LAYERS, 3, width)
    gathered = lax.all_gather(after(params, turned), ("h", "c"), axis=2, tiled=True)
    params = gathered.reshape(LAYERS, 3, blocks, LANES)
    share = after(share, gathered, valid)
    own += [swap(piece, 2 + i) for i, piece in enumerate(after(pieces[2:], share))]
    far = assemble(place, [plane_gather(share)])
    own = own[:2] + after(own[2:], far)
    others += [swap_half(piece) for piece in own[2:]]
    half_weights = [[weights, near, far, swap(far, 1)]]
    share = lax.ppermute(after(far_share(1), own), "h", FLIP2)

    upstream = None
    saved = []
    chunk_plan = (2, 1)
    for layer in range(LAYERS):
        flat = layer == 0
        other = others
        if layer > 0:
            other = [swap_half(piece) for piece in own]
        z, *own_flat = project(own_blocks, place, own, half_weights[layer], layer, flat=flat)
        if layer == LAYERS - 1:
            turned = after(turned, z)
            upstream = [swap(piece, rel) for rel, piece in enumerate(turned)]
        z, stats, *other_flat = project(
            other_blocks, place, other, half_weights[layer], layer, z, valid, flat=flat
        )
        if layer == 0:
            plane = lax.all_gather(stats, ("y", "x"))
            far = lax.all_gather(after(share, plane), ("y", "x"), axis=0, tiled=True)
            stats = lax.all_gather(plane, ("h", "c")).reshape(16, *stats.shape)
        else:
            stats = gather_sums(stats)
        chunks = chunk_plan[layer]
        pieces = 4 if layer == LAYERS - 1 else 1
        state = jnp.zeros((blocks, LANES), F32)
        following, states, slopes = [], [], []
        for chunk in range(chunks):
            *new, kept, slope, state = recur(
                chunk, chunks, place, gate, z, stats, params[layer], valid, state, own, pieces
            )
            following.extend(new)
            states.append(kept)
            slopes.append(slope)
        if layer == 0:
            groups = [own_flat, other_flat]
            groups += [[swap(after(p, state), 1) for p in group] for group in groups]
            x_split = prepare(all_blocks, groups)
            half_weights.append([weights, near, far, swap(after(far, x_split), 1)])
        else:
            groups = [own, other]
            groups += [[swap(after(p, z), 1) for p in group] for group in groups]
            x_split = None
        saved.append((groups, x_split, z, stats, states, slopes))
        own = following
    output = [swap(piece, rel) for rel, piece in enumerate(own)]

    ups = upstream
    results = [None] * LAYERS

    def next_step(totals, swapper, *before):
        return [(t[0], swapper(t[1])) for t in totals]

    def add_up(pairs, *before):
        return [kept + after(come, *before) for kept, come in pairs]

    def over_second(array):
        return plane_swap(array, 1)

    def over_h(array):
        return lax.ppermute(array, "h", FLIP2)

    waiting = None
    for layer in range(LAYERS - 1, -1, -1):
        groups, x_split, z, stats, states, slopes = saved[layer]
        weight = half_weights[layer]
        grad_pre, sums = back(place, gate, z, stats, params[layer], ups, states, slopes)
        if waiting is not None:
            totals = add_up(waiting, grad_pre)
            sums = after(sums, totals)
            waiting = next_step(totals, over_second)
        sums = gather_sums(sums)
        grad_z, leaving, near_terms, far_terms, sums = norm_back(
            other_columns, place, grad_pre, z, params[layer], valid, stats, sums, weight, layer
        )
        received = [swap_half(far_terms)]
        leaving = swap(leaving, 1)
        if waiting is not None:
            totals = add_up(waiting, grad_z)
            leaving = after(leaving, totals)
            waiting = next_step(totals, over_h)
        if x_split is None:
            received = [swap_half(near_terms)] + received
            x_split = prepare(all_blocks, after(groups, grad_z))
        sent, *g_split = leaving_rows(0, place, (grad_z, leaving), x_split, width)
        come = [plane_swap(sent, 0)]
        (sent,) = leaving_rows(1, place, g_split, x_split, width)
        come.append(plane_swap(sent, 0))
        if layer == 0:
            received = [swap_half(after(near_terms, received, sent))] + received
        kept = own_terms(own_columns, place, after(grad_z, sent), ups, weight, layer)
        ups = [kept, *received]
        if layer > 0:
            stay = staying_rows(after(g_split, kept), x_split, width)
            half = depth // 2
            waiting = [(stay[..., :half], come[0]), (stay[..., half:], come[1])]
        results[layer] = lax.dynamic_index_in_dim(
            sums.reshape(3, 4, width), clip, axis=1, keepdims=False
        )

    def grad_piece(rel):
        other = received[rel // 2]
        at = (rel % 2) * width
        return kept[:, rel * width : (rel + 1) * width] + other[:, at : at + width]

    far = [grad_piece(2), grad_piece(3)]
    grad_in = [swap(piece, 2 + i) for i, piece in enumerate(far)]
    stay = staying_rows(after(g_split, far), x_split, width)
    half = depth // 2
    totals = add_up([(stay[..., :half], come[0]), (stay[..., half:], come[1])])
    later = waiting
    waiting = next_step(totals, over_second)
    received[0] = after(received[0], totals)
    close = [grad_piece(0), grad_piece(1)]
    grad_in = [close[0], swap(close[1], 1)] + grad_in
    totals = add_up(waiting, close)
    waiting = next_step(totals, over_h)
    later = jnp.concatenate(add_up(later, totals), axis=1)
    later = lax.all_gather(later, ("y", "x"), axis=0, tiled=True)
    output = unpack(place, after(output, totals))
    shares = add_up(waiting, output)
    gathered = [plane_gather(share) for share in shares]
    grad_in = unpack(place, after(grad_in, shares))
    grad_weights = keep(after(later, grad_in), 1)
    grad_weights = assemble(place, gathered, 0, grad_weights)
    sums = jnp.stack(results)
    return (
        output,
        grad_in,
        grad_weights,
        sums[:, 0],
        sums[:, 1],
        sums[:, 2],
        sums[:, 1],
    )


def gelu_slope(value):
    return (
        0.5 * (1.0 + jax.scipy.special.erf(value / ROOT_TWO))
        + value * jnp.exp(-0.5 * value * value) / ROOT_TWO_PI
    )


def recur_step(decay, state, inputs):
    drive_t, valid_t = inputs
    pre = drive_t + decay * state
    state = state + valid_t * (jax.nn.gelu(pre, approximate=False) - state)
    return (state, state)


def back_step(decay, carry, inputs):
    upstream_t, valid_t, pre_t = inputs
    total = upstream_t + carry
    grad_pre = total * valid_t * gelu_slope(pre_t)
    carry = total * (1.0 - valid_t) + grad_pre * decay
    return (carry, grad_pre)


def add_piece(weight, piece):
    return jnp.dot(weight, piece, precision=HIGH, preferred_element_type=jnp.float32)


def weight_columns(grad_pre_norm, piece):
    return jnp.einsum("jf,kf->jk", grad_pre_norm, piece, precision=HIGH)


def split_features(inputs, weights, gains, shifts, decays, biases, lengths, frame_mask, grad_out):
    width, slots = inputs.shape
    clips, frames_len = frame_mask.shape
    frames = jnp.arange(frames_len, dtype=jnp.int32)
    valid_grid = (
        (frames[None, :] < lengths[:, None]) & ((frame_mask == 1) | (frames[None, :] == 0))
    ).astype(jnp.float32)
    valid = valid_grid.reshape(-1)
    valid_row = valid[None, :]
    valid_time = jnp.broadcast_to(valid_grid.T[:, :, None], (frames_len, clips, width)).reshape(
        frames_len, clips * width
    )
    count_local = jnp.sum(valid)

    def to_time(array):
        return jnp.transpose(array.reshape(width, clips, frames_len), (2, 1, 0)).reshape(
            frames_len, clips * width
        )

    def from_time(array):
        return jnp.transpose(array.reshape(frames_len, clips, width), (2, 1, 0)).reshape(
            width, slots
        )

    layer_in = inputs
    saved = []
    for layer_no in range(LAYERS):
        weight = weights[layer_no]
        gathered = lax.all_gather(layer_in, "neuron", axis=0, tiled=True)
        pre_norm = add_piece(weight, gathered)
        first_sum, count = lax.psum((jnp.sum(valid_row * pre_norm, axis=1), count_local), "batch")
        mean = first_sum / count
        centered = pre_norm - mean[:, None]
        var = lax.psum(jnp.sum(valid_row * centered * centered, axis=1), "batch") / count
        inv_std = lax.rsqrt(var + EPS)
        zhat = (pre_norm - mean[:, None]) * inv_std[:, None]
        drive = gains[layer_no][:, None] * zhat + (shifts[layer_no] + biases[layer_no])[:, None]
        drive_time = to_time(drive)
        decay_wide = jnp.tile(decays[layer_no], clips)
        start_state = jnp.zeros((clips * width,), jnp.float32)
        _, states = lax.scan(
            partial(recur_step, decay_wide), start_state, (drive_time, valid_time), unroll=8
        )
        saved.append((gathered, zhat, inv_std, drive_time, states, count))
        layer_in = layer_in + valid_row * from_time(states)
    upstream = grad_out
    grad_parts = [None] * LAYERS
    for layer_no in range(LAYERS - 1, -1, -1):
        gathered, zhat, inv_std, drive_time, states, count = saved[layer_no]
        decay_wide = jnp.tile(decays[layer_no], clips)
        gain = gains[layer_no]
        previous = jnp.concatenate([jnp.zeros_like(states[:1]), states[:-1]], axis=0)
        pre_time = drive_time + decay_wide[None, :] * previous
        grad_state = to_time(valid_row * upstream)
        start_carry = jnp.zeros((clips * width,), jnp.float32)
        _, grad_pre_time = lax.scan(
            partial(back_step, decay_wide),
            start_carry,
            (grad_state, valid_time, pre_time),
            reverse=True,
            unroll=8,
        )
        decay_local = jnp.sum(
            jnp.sum(grad_pre_time * previous, axis=0).reshape(clips, width), axis=0
        )
        grad_pre = from_time(grad_pre_time)
        gain_local = jnp.sum(grad_pre * zhat, axis=1)
        shift_local = jnp.sum(grad_pre, axis=1)
        grad_gain, grad_shift, grad_decay = lax.psum(
            (gain_local, shift_local, decay_local), "batch"
        )
        grad_pre_norm = (gain * inv_std)[:, None] * (
            grad_pre - valid_row * (grad_shift[:, None] + zhat * grad_gain[:, None]) / count
        )
        weight_local = weight_columns(grad_pre_norm, gathered)
        input_terms = jnp.einsum("jk,jf->kf", weights[layer_no], grad_pre_norm, precision=HIGH)
        input_grad = lax.psum_scatter(input_terms, "neuron", scatter_dimension=0, tiled=True)
        grad_weight = lax.psum(weight_local, "batch")
        upstream = upstream + input_grad
        grad_parts[layer_no] = (grad_weight, grad_gain, grad_shift, grad_decay)
    grad_weights = jnp.stack([grad_parts[layer_no][0] for layer_no in range(LAYERS)])
    grad_gains = jnp.stack([grad_parts[layer_no][1] for layer_no in range(LAYERS)])
    grad_shifts = jnp.stack([grad_parts[layer_no][2] for layer_no in range(LAYERS)])
    grad_decays = jnp.stack([grad_parts[layer_no][3] for layer_no in range(LAYERS)])
    return (layer_in, upstream, grad_weights, grad_gains, grad_shifts, grad_decays, grad_shifts)


def solution(mesh):
    if (mesh.shape["batch"], mesh.shape["neuron"]) == (4, 8):
        cut = Mesh(mesh.devices.reshape(2, 2, 2, 2, 2), ("y", "x", "h", "l", "c"))
        batch, neuron, body = ("y", "x"), ("h", "l", "c"), half_features
    else:
        cut, batch, neuron, body = mesh, "batch", "neuron", split_features
    in_specs = (
        P(neuron, batch),
        P(None, neuron, None),
        P(None, neuron),
        P(None, neuron),
        P(None, neuron),
        P(None, neuron),
        P(batch),
        P(batch, None),
        P(neuron, batch),
    )
    out_specs = (
        P(neuron, batch),
        P(neuron, batch),
        P(None, neuron, None),
        P(None, neuron),
        P(None, neuron),
        P(None, neuron),
        P(None, neuron),
    )
    return jax.shard_map(
        body, mesh=cut, in_specs=in_specs, out_specs=out_specs, check_vma=False
    )
```

```python
from functools import partial
import math

import jax
import jax.numpy as jnp
from jax import lax
from jax.experimental import pallas as pl
from jax.experimental.pallas import tpu as pltpu
from jax.sharding import Mesh, PartitionSpec as P

LAYERS = 2
EPS = 1e-05
HIGH = lax.Precision.HIGHEST
ROOT_TWO = math.sqrt(2.0)
ROOT_TWO_PI = math.sqrt(2.0 * math.pi)
F32 = jnp.float32
BF16 = jnp.bfloat16
LANES = 128
VMEM_LIMIT = 48 * 1024 * 1024
SMEM_SPEC = pl.BlockSpec(memory_space=pltpu.SMEM)
VMEM_SPEC = pl.BlockSpec(memory_space=pltpu.VMEM)


FLIP2 = [(0, 1), (1, 0)]


def swap_half(array):
    return lax.ppermute(array, "l", FLIP2)


def split(value):
    high = value.astype(BF16)
    return high, (value - high.astype(F32)).astype(BF16)


def dot(a, b, dims):
    return lax.dot_general(a, b, (dims, ((), ())), preferred_element_type=F32)


NT = ((1,), (1,))
NN = ((1,), (0,))


def call(body, **kwargs):
    return pl.pallas_call(
        body,
        compiler_params=pltpu.CompilerParams(vmem_limit_bytes=VMEM_LIMIT),
        **kwargs,
    )


def cost(flops, byte_count):
    return pl.CostEstimate(flops=int(flops) // 64, bytes_accessed=int(byte_count) // 64, transcendentals=0)


def pack_body(frames, place_ref, in_ref, near_ref, far_ref, turned):
    slots = in_ref.shape[1]
    for start in range(0, slots, LANES):
        turned[start : start + LANES, :] = in_ref[:, start : start + LANES].T
    for rel in range(4):
        first = pl.multiple_of(place_ref[rel] * frames, 8)
        out = (near_ref, far_ref)[rel // 2]
        out[(rel % 2) * frames : (rel % 2 + 1) * frames, :] = turned[pl.ds(first, frames), :]


def pack(place, array, frames):
    width, slots = array.shape
    return call(
        partial(pack_body, frames),
        out_shape=[jax.ShapeDtypeStruct((2 * frames, width), F32)] * 2,
        in_specs=[SMEM_SPEC, VMEM_SPEC],
        out_specs=[VMEM_SPEC] * 2,
        scratch_shapes=[pltpu.VMEM((slots, width), F32)],
        cost_estimate=cost(0, 8 * width * slots),
        name="pack",
    )(place, array)


def part_spec(part, frames):
    array, i = part
    if i is None:
        return pl.BlockSpec(array.shape, lambda *_: (0,) * array.ndim)
    return pl.BlockSpec((frames, array.shape[1]), lambda *_: (i, 0))


def arrays_of(parts):
    return [array for array, _ in parts]


def unpack_body(frames, place_ref, *refs):
    ins, out_ref, turned = refs[:4], refs[4], refs[5]
    slots = out_ref.shape[1]
    for rel in range(4):
        first = pl.multiple_of(place_ref[rel] * frames, 8)
        turned[pl.ds(first, frames), :] = ins[rel][...]
    for start in range(0, slots, LANES):
        out_ref[:, start : start + LANES] = turned[start : start + LANES, :].T


def unpack(place, parts, frames):
    width = parts[0][0].shape[1]
    slots = 4 * frames
    return call(
        partial(unpack_body, frames),
        grid=(1,),
        out_shape=jax.ShapeDtypeStruct((width, slots), F32),
        in_specs=[SMEM_SPEC] + [part_spec(part, frames) for part in parts],
        out_specs=pl.BlockSpec((width, slots), lambda i: (0, 0)),
        scratch_shapes=[pltpu.VMEM((slots, width), F32)],
        cost_estimate=cost(0, 8 * width * slots),
        name="unpack",
    )(place, *arrays_of(parts))


def merge_body(kept_ref, come_ref, out_ref):
    frames, columns = kept_ref.shape
    width = columns // 2
    for i in range(2):
        some = slice(i * width, (i + 1) * width)
        out_ref[i * frames : (i + 1) * frames, :] = kept_ref[:, some] + come_ref[:, some]


def merge(kept, half, come):
    frames, columns = come.shape
    return call(
        merge_body,
        grid=(1,),
        out_shape=jax.ShapeDtypeStruct((2 * frames, columns // 2), F32),
        in_specs=[
            pl.BlockSpec((frames, columns), lambda i: (0, half)),
            pl.BlockSpec((frames, columns), lambda i: (0, 0)),
        ],
        out_specs=pl.BlockSpec((2 * frames, columns // 2), lambda i: (0, 0)),
        cost_estimate=cost(0, 12 * frames * columns),
        name="merge",
    )(kept, come)


def spread_of(parts, width):
    spots, row, column = [], 0, 0
    for array, _ in parts:
        spots.append((row, column))
        if array.shape[1] == width:
            column += width
        else:
            row += array.shape[0]
    return spots


def project_body(n_parts, spots, with_acc, with_stats, flat, cols_ref, place_ref, *refs):
    del cols_ref
    parts, refs = refs[:n_parts], refs[n_parts:]
    weights, refs = refs[:4], refs[4:]
    if with_acc:
        acc_ref, refs = refs[0], refs[1:]
    if with_stats:
        valid_ref, refs = refs[0], refs[1:]
    out_ref, refs = refs[0], refs[1:]
    if with_stats:
        stats_ref, refs = refs[0], refs[1:]
    if flat:
        flat_ref, refs = refs[0], refs[1:]
    x_high, x_low = refs
    step = pl.program_id(0)
    width = x_high.shape[2]

    @pl.when(step == 0)
    def _():
        for (row, column), part in zip(spots, parts):
            rows, columns = part.shape
            for start in range(0, columns, width):
                rel = (column + start) // width
                high, low = split(part[:, start : start + width])
                x_high[rel, row : row + rows, :] = high
                x_low[rel, row : row + rows, :] = low
            if flat:
                flat_ref[row : row + rows, column : column + columns] = part[...]
        if with_acc:
            out_ref[...] = acc_ref[...]
        else:
            out_ref[...] = jnp.zeros_like(out_ref)

    stacked = jnp.concatenate([x_high[step], x_low[step], x_high[step]], axis=1)
    for block in range(4):
        w_high, w_low = split(weights[block][...].reshape(width, width))
        columns = slice(block * width, (block + 1) * width)
        out_ref[:, columns] += dot(stacked, jnp.concatenate([w_high, w_high, w_low], axis=1), NT)

    if with_stats:

        @pl.when(step == pl.num_programs(0) - 1)
        def _():
            valid = valid_ref[...]
            own = jnp.sum(valid, axis=0, keepdims=True)
            per = width // LANES
            for row in range(out_ref.shape[1] // LANES):
                z = out_ref[:, row * LANES : (row + 1) * LANES]
                total = jnp.sum(valid * z, axis=0, keepdims=True)
                centred = valid * (z - total / own)
                squares = jnp.sum(centred * centred, axis=0, keepdims=True)
                at = place_ref[row // per] * per + row % per
                stats_ref[0, pl.ds(at, 1), :] = total
                stats_ref[1, pl.ds(at, 1), :] = squares
                stats_ref[2, pl.ds(at, 1), :] = own


def weight_specs(weights, layer, pairs=2):
    specs = []
    for weight in weights:
        width = weight.shape[-2]
        if weight.ndim == 3:
            specs.append(
                pl.BlockSpec((1, width, pairs * width), lambda s, cols, *_: (layer, 0, cols[s]))
            )
        else:
            specs.append(pl.BlockSpec((width, pairs * width), lambda s, cols, *_: (0, cols[s])))
    return specs


def project(columns, place, frames, parts, weights, layer, acc=None, valid=None, flat=False):
    width = weights[0].shape[-2]
    full = pl.BlockSpec(memory_space=pltpu.VMEM)
    in_specs = [part_spec(part, frames) for part in parts]
    in_specs += weight_specs(weights, layer, 1)
    operands = arrays_of(parts) + list(weights)
    array = jax.ShapeDtypeStruct((frames, 4 * width), F32)
    array_spec = pl.BlockSpec((frames, 4 * width), lambda s, cols, place: (0, 0))
    out_shape, out_specs = [array], [array_spec]
    if acc is not None:
        in_specs.append(full)
        operands.append(acc)
    if valid is not None:
        in_specs.append(full)
        operands.append(valid)
        rows = 4 * width // LANES
        out_shape.append(jax.ShapeDtypeStruct((3, rows, LANES), F32))
        out_specs.append(pl.BlockSpec((3, rows, LANES), lambda s, cols, place: (0, 0, 0)))
    if flat:
        out_shape.append(array)
        out_specs.append(array_spec)
    return call(
        partial(
            project_body,
            len(parts),
            spread_of(parts, width),
            acc is not None,
            valid is not None,
            flat,
        ),
        grid_spec=pltpu.PrefetchScalarGridSpec(
            num_scalar_prefetch=2,
            grid=(4,),
            in_specs=in_specs,
            out_specs=out_specs,
            scratch_shapes=[pltpu.VMEM((4, frames, width), BF16)] * 2,
        ),
        out_shape=out_shape,
        cost_estimate=cost(2 * 3 * frames * 16 * width * width, 4 * 16 * width * width),
        name="project",
    )(columns, place, *operands)


def to_relative(place_ref, spread, rows_ref, value, slot):
    per = value.shape[0] // 4
    spread[...] = value
    for rel in range(4):
        first = place_ref[rel] * per
        for row in range(per):
            rows_ref[slot, rel * per + row : rel * per + row + 1, :] = spread[
                pl.ds(first + row, 1), :
            ]


def tree(values):
    while len(values) > 1:
        values = [a + b for a, b in zip(values[::2], values[1::2])]
    return values[0]


def norm_terms(stats_ref):
    each = [[stats_ref[i, slot] for i in range(stats_ref.shape[0])] for slot in range(3)]
    totals, squares, owns = each
    count = tree(owns)
    mean = tree(totals) / count
    away = [total / own - mean for total, own in zip(totals, owns)]
    spread = tree([s + n * a * a for s, n, a in zip(squares, owns, away)])
    return count, mean, lax.rsqrt(spread / count + EPS)


def recur_body(n_parts, spots, n_out, first, place_ref, gate_ref, z_ref, stats_ref, params_ref, valid_ref, start_ref, *refs):
    parts, refs = refs[:n_parts], refs[n_parts:]
    outs, refs = refs[:n_out], refs[n_out:]
    state_ref, slope_ref, last_ref, rows, spread, drive_s, state_s, slope_s = refs
    frames = z_ref.shape[0]
    blocks = z_ref.shape[1] // LANES
    _, mean, inv_std = norm_terms(stats_ref)
    to_relative(place_ref, spread, rows, mean, 0)
    to_relative(place_ref, spread, rows, params_ref[0] * inv_std, 1)
    to_relative(place_ref, spread, rows, params_ref[1], 2)
    to_relative(place_ref, spread, rows, params_ref[2], 3)
    for row in range(blocks):
        z = z_ref[:, row * LANES : (row + 1) * LANES]
        drive_s[row * frames : (row + 1) * frames, :] = (
            z - rows[0, row : row + 1, :]
        ) * rows[1, row : row + 1, :] + rows[2, row : row + 1, :]
    decay = rows[3]

    def step(t, state):
        at = pl.ds(t, blocks, stride=frames)
        pre = drive_s[at, :] + decay * state
        half = 0.5 + 0.5 * lax.erf(pre * (1.0 / ROOT_TWO))
        gate = gate_ref[first + t] > 0.0
        slope = half + pre * jnp.exp(-0.5 * pre * pre) * (1.0 / ROOT_TWO_PI)
        state = jnp.where(gate, pre * half, state)
        state_s[at, :] = state
        slope_s[at, :] = jnp.where(gate, slope, 0.0)
        return state

    last_ref[...] = lax.fori_loop(0, frames, step, start_ref[...], unroll=8)
    valid = valid_ref[...]
    for row in range(blocks):
        lanes = slice(row * LANES, (row + 1) * LANES)
        state = state_s[row * frames : (row + 1) * frames, :]
        state_ref[:, lanes] = state
        slope_ref[:, lanes] = slope_s[row * frames : (row + 1) * frames, :]
        for (top, column), part in zip(spots, parts):
            if column <= row * LANES < column + part.shape[1]:
                x = part[:, row * LANES - column : (row + 1) * LANES - column]
                some = slice(top, top + part.shape[0])
                out, base, at = outs[0], top, row * LANES
                if len(outs) > 1:
                    rel, inner = divmod(row * LANES, outs[0].shape[1])
                    out, base, at = outs[rel // 2], (rel % 2) * frames + top, inner
                out[base : base + part.shape[0], at : at + LANES] = x + valid[some] * state[some]


def recur(chunk, chunks, place, gate, z, stats, params, valid, start, parts, last):
    frames = z.shape[0] // chunks
    features = z.shape[1]
    width = features // 4
    blocks = features // LANES
    row_block = lambda columns: pl.BlockSpec((frames, columns), lambda i: (chunk, 0))
    whole = lambda array: pl.BlockSpec(array.shape, lambda i: (0,) * array.ndim)
    part_specs = []
    for array, at in parts:
        if at is None:
            part_specs.append(whole(array))
        else:
            part_specs.append(
                pl.BlockSpec((frames, width), lambda i, at=at: (at * chunks + chunk, 0))
            )
    tile = jax.ShapeDtypeStruct((blocks, LANES), F32)
    full = jax.ShapeDtypeStruct((frames, features), F32)
    outs = [jax.ShapeDtypeStruct((2 * frames, width), F32)] * 2 if last else [full]
    out_shape = outs + [full, full, tile]
    return call(
        partial(recur_body, len(parts), spread_of(parts, width), len(outs), chunk * frames),
        grid=(1,),
        in_specs=[
            SMEM_SPEC,
            SMEM_SPEC,
            row_block(features),
            whole(stats),
            whole(params),
            row_block(LANES),
            whole(start),
        ]
        + part_specs,
        out_specs=[whole(s) for s in out_shape],
        out_shape=out_shape,
        scratch_shapes=[
            pltpu.VMEM((4, blocks, LANES), F32),
            pltpu.VMEM((blocks, LANES), F32),
        ]
        + [pltpu.VMEM((blocks * frames, LANES), F32)] * 3,
        cost_estimate=cost(100 * frames * features, 20 * frames * features),
        name="recur",
    )(place, gate, z, stats, params, valid, start, *arrays_of(parts))


def back_body(n_parts, spots, n_state, place_ref, gate_ref, z_ref, stats_ref, params_ref, *refs):
    parts, refs = refs[:n_parts], refs[n_parts:]
    states, refs = refs[:n_state], refs[n_state:]
    slopes, refs = refs[:n_state], refs[n_state:]
    grad_ref, sums_ref, rows, spread, up_s, state_s, slope_s = refs
    frames = z_ref.shape[0]
    blocks = z_ref.shape[1] // LANES
    tall = frames + 8
    _, mean, inv_std = norm_terms(stats_ref)
    to_relative(place_ref, spread, rows, mean, 0)
    to_relative(place_ref, spread, rows, inv_std, 1)
    to_relative(place_ref, spread, rows, params_ref[2], 2)
    for row in range(blocks):
        lanes = slice(row * LANES, (row + 1) * LANES)
        base = row * frames
        up = None
        for (top, column), part in zip(spots, parts):
            if column <= row * LANES < column + part.shape[1] and part.shape[0] == frames:
                value = part[:, row * LANES - column : (row + 1) * LANES - column]
                up = value if up is None else up + value
        up_s[base : base + frames, :] = up
        state_s[row * tall : row * tall + 8, :] = jnp.zeros((8, LANES), F32)
        first = 0
        for state, slope in zip(states, slopes):
            some = state.shape[0]
            at = row * tall + 8 + first
            state_s[at : at + some, :] = state[:, lanes]
            slope_s[base + first : base + first + some, :] = slope[:, lanes]
            first += some
    decay = rows[2]

    def step(i, carry):
        t = frames - 1 - i
        at = pl.ds(t, blocks, stride=frames)
        slope = slope_s[at, :]
        gate = gate_ref[t]
        total = gate * up_s[at, :] + carry
        up_s[at, :] = total * slope
        return total * (slope * decay + (1.0 - gate))

    lax.fori_loop(0, frames, step, jnp.zeros((blocks, LANES), F32), unroll=8)
    per = blocks // 4
    for row in range(blocks):
        lanes = slice(row * LANES, (row + 1) * LANES)
        base = row * frames
        grad = up_s[base : base + frames, :]
        grad_ref[:, lanes] = grad
        zhat = (z_ref[:, lanes] - rows[0, row : row + 1, :]) * rows[1, row : row + 1, :]
        before = state_s[row * tall + 7 : row * tall + 7 + frames, :]
        at = place_ref[row // per] * per + row % per
        for slot, value in enumerate((grad * zhat, grad, grad * before)):
            sums_ref[slot, pl.ds(at, 1), :] = jnp.sum(value, axis=0, keepdims=True)


def spots_of_sum(parts, width):
    spots, column = [], 0
    for array, _ in parts:
        spots.append((0, column % (4 * width)))
        column += array.shape[1]
    return spots


def back(place, gate, z, stats, params, ups, states, slopes):
    frames, features = z.shape
    width = features // 4
    blocks = features // LANES
    whole = lambda array: pl.BlockSpec(array.shape, lambda i: (0,) * array.ndim)
    out_shape = [
        jax.ShapeDtypeStruct((frames, features), F32),
        jax.ShapeDtypeStruct((3, blocks, LANES), F32),
    ]
    return call(
        partial(back_body, len(ups), spots_of_sum(ups, width), len(states)),
        grid=(1,),
        in_specs=[SMEM_SPEC] * 2
        + [whole(a) for a in (z, stats, params)]
        + [part_spec(up, frames) for up in ups]
        + [whole(a) for a in (*states, *slopes)],
        out_specs=[whole(a) for a in out_shape],
        out_shape=out_shape,
        scratch_shapes=[
            pltpu.VMEM((3, blocks, LANES), F32),
            pltpu.VMEM((blocks, LANES), F32),
            pltpu.VMEM((blocks * frames, LANES), F32),
            pltpu.VMEM((blocks * (frames + 8), LANES), F32),
            pltpu.VMEM((blocks * frames, LANES), F32),
        ],
        cost_estimate=cost(30 * frames * features, 20 * frames * features),
        name="back",
    )(place, gate, z, stats, params, *arrays_of(ups), *states, *slopes)


def input_terms(high_s, low_s, weights):
    width = high_s.shape[2]
    left, right = [], []
    for block, weight in enumerate(weights):
        w_high, w_low = split(weight[...].reshape(width, 2 * width))
        left += [high_s[block], low_s[block], high_s[block]]
        right += [w_high, w_high, w_low]
    return dot(jnp.concatenate(left, axis=1), jnp.concatenate(right, axis=0), NN)


def norm_back_body(split_terms, cols_ref, place_ref, grad_ref, z_ref, params_ref, valid_ref, stats_ref, sums_ref, *refs):
    del cols_ref
    weights, refs = refs[:4], refs[4:]
    if split_terms:
        out_ref, leave_ref, near_term_ref, far_term_ref, sums_out_ref, *refs = refs
        term_refs, starts = (far_term_ref, near_term_ref), (0, 0)
    else:
        out_ref, leave_ref, term_ref, sums_out_ref, *refs = refs
        term_refs, starts = (term_ref, term_ref), (2 * grad_ref.shape[1] // 4, 0)
    rows, spread, high_s, low_s = refs
    blocks = z_ref.shape[1] // LANES
    width = high_s.shape[2]
    per = width // LANES

    @pl.when(pl.program_id(0) == 0)
    def _():
        count, mean, inv_std = norm_terms(stats_ref)
        to_relative(place_ref, spread, rows, mean, 0)
        to_relative(place_ref, spread, rows, inv_std, 1)
        to_relative(place_ref, spread, rows, params_ref[0] * inv_std, 2)
        sums = tree([sums_ref[i] for i in range(sums_ref.shape[0])])
        sums_out_ref[...] = sums
        to_relative(place_ref, spread, rows, sums[0] / count, 3)
        to_relative(place_ref, spread, rows, sums[1] / count, 4)
        valid = valid_ref[...]
        for row in range(blocks):
            lanes = slice(row * LANES, (row + 1) * LANES)
            one = lambda slot: rows[slot, row : row + 1, :]
            zhat = (z_ref[:, lanes] - one(0)) * one(1)
            value = one(2) * (grad_ref[:, lanes] - valid * (one(4) + zhat * one(3)))
            out_ref[:, lanes] = value
            if (row // per) % 2:
                at = (row // per // 2) * width + (row % per) * LANES
                leave_ref[:, at : at + LANES] = value
            high, low = split(value)
            inner = slice((row % per) * LANES, (row % per + 1) * LANES)
            high_s[row // per, :, inner] = high
            low_s[row // per, :, inner] = low

    value = input_terms(high_s, low_s, weights)
    for step, (term_ref, first) in enumerate(zip(term_refs, starts)):

        @pl.when(pl.program_id(0) == step)
        def _():
            for pair in range(2):
                at = pl.multiple_of(((place_ref[0] & 1) ^ pair) * width, width)
                term_ref[:, pl.ds(first + at, width)] = value[
                    :, pair * width : (pair + 1) * width
                ]


def norm_back(columns, place, grad, z, params, valid, stats, sums, weights, layer, split_terms):
    frames, features = z.shape
    width = features // 4
    blocks = features // LANES
    whole = lambda array: pl.BlockSpec(array.shape, lambda s, cols, place: (0,) * array.ndim)
    operands = [grad, z, params, valid, stats, sums]
    full = jax.ShapeDtypeStruct((frames, features), F32)
    half = jax.ShapeDtypeStruct((frames, 2 * width), F32)
    terms = [half, half] if split_terms else [full]
    out_shape = [full, half, *terms, jax.ShapeDtypeStruct((3, blocks, LANES), F32)]
    return call(
        partial(norm_back_body, split_terms),
        grid_spec=pltpu.PrefetchScalarGridSpec(
            num_scalar_prefetch=2,
            grid=(2,),
            in_specs=[whole(a) for a in operands] + weight_specs(weights, layer),
            out_specs=[whole(a) for a in out_shape],
            scratch_shapes=[
                pltpu.VMEM((5, blocks, LANES), F32),
                pltpu.VMEM((blocks, LANES), F32),
                pltpu.VMEM((4, frames, width), BF16),
                pltpu.VMEM((4, frames, width), BF16),
            ],
        ),
        out_shape=out_shape,
        cost_estimate=cost(6 * frames * features * features, 4 * features * features),
        name="norm_back",
    )(columns, place, *operands, *weights)


def own_terms_body(n_ups, spots, cols_ref, place_ref, grad_ref, *refs):
    del cols_ref
    ups, refs = refs[:n_ups], refs[n_ups:]
    weights, refs = refs[:4], refs[4:]
    out_ref, high_s, low_s = refs
    width = high_s.shape[2]
    step = pl.program_id(0)

    @pl.when(step == 0)
    def _():
        for block in range(4):
            high, low = split(grad_ref[:, block * width : (block + 1) * width])
            high_s[block] = high
            low_s[block] = low

    value = input_terms(high_s, low_s, weights)
    for pair in range(2):
        at = pl.multiple_of(((place_ref[0] & 1) ^ pair) * width, width)
        out_ref[:, pl.ds(at, width)] = value[:, pair * width : (pair + 1) * width]
    for half in range(2):

        @pl.when(step == half)
        def _():
            first = 2 * half * width
            for (_, column), up in zip(spots, ups):
                low = max(column, first)
                high = min(column + up.shape[1], first + 2 * width)
                if low < high:
                    out_ref[:, low - first : high - first] += up[:, low - column : high - column]


def own_terms(columns, place, grad, ups, weights, layer):
    frames, features = grad.shape
    width = features // 4
    whole = lambda array: pl.BlockSpec(array.shape, lambda s, cols, place: (0,) * array.ndim)
    step_block = pl.BlockSpec((frames, 2 * width), lambda s, cols, place: (0, s))
    return call(
        partial(own_terms_body, len(ups), spots_of_sum(ups, width)),
        grid_spec=pltpu.PrefetchScalarGridSpec(
            num_scalar_prefetch=2,
            grid=(2,),
            in_specs=[whole(grad)]
            + [part_spec(up, frames) for up in ups]
            + weight_specs(weights, layer),
            out_specs=step_block,
            scratch_shapes=[pltpu.VMEM((4, frames, width), BF16)] * 2,
        ),
        out_shape=jax.ShapeDtypeStruct((frames, features), F32),
        cost_estimate=cost(6 * frames * features * features, 4 * features * features),
        name="own_terms",
    )(columns, place, grad, *arrays_of(ups), *weights)


def prepare_body(n_chunks, lists_ref, *refs):
    del lists_ref
    groups = []
    for _ in range(4):
        groups.append(refs[:n_chunks])
        refs = refs[n_chunks:]
    high_ref, low_ref = refs
    padded = high_ref.shape[0] // 2
    for side in range(2):

        @pl.when(pl.program_id(0) // 4 == side)
        def _():
            for clip in range(2):
                row = clip * padded
                for part in groups[2 * clip + side]:
                    rows = part.shape[0]
                    high, low = split(part[...])
                    high_ref[row : row + rows, :] = high
                    low_ref[row : row + rows, :] = low
                    row += rows
                rest = (clip + 1) * padded - row
                zeros = jnp.zeros((rest, high_ref.shape[1]), BF16)
                high_ref[row : row + rest, :] = zeros
                low_ref[row : row + rest, :] = zeros


def prepare(lists, groups):
    width = groups[0][0].shape[1] // 4
    frames = sum(part.shape[0] for part in groups[0])
    padded = -(-frames // LANES) * LANES
    in_specs = []
    for i, group in enumerate(groups):
        for part in group:
            if i % 2 == 0:
                index = lambda s, cols, flip=i // 2: (0, jnp.minimum(s, 3) ^ flip)
            else:
                index = lambda s, cols, flip=i // 2: (0, jnp.maximum(s - 4, 0) ^ flip)
            in_specs.append(pl.BlockSpec((part.shape[0], width), index))
    out = jax.ShapeDtypeStruct((2 * padded, 8 * width), BF16)
    return call(
        partial(prepare_body, len(groups[0])),
        grid_spec=pltpu.PrefetchScalarGridSpec(
            num_scalar_prefetch=1,
            grid=(8,),
            in_specs=in_specs,
            out_specs=[pl.BlockSpec((2 * padded, width), lambda s, cols: (0, cols[s]))] * 2,
        ),
        out_shape=[out, out],
        cost_estimate=cost(0, 16 * frames * 8 * width),
        name="prepare",
    )(lists, *[part for group in groups for part in group])


def product(g_high, g_low, x_high, x_low):
    return dot(g_high, x_high, NN) + (dot(g_high, x_low, NN) + dot(g_low, x_high, NN))


def leaving_body(turn, place_ref, *refs):
    if turn:
        grad_ref, near_ref, x_high, x_low, sent, g_high, g_low, t_high, t_low = refs

        @pl.when(pl.program_id(0) == 0)
        def _():
            frames, features = grad_ref.shape
            width = features // 4
            rows = width // 4
            padded = t_high.shape[1] // 2
            t_high[...] = jnp.zeros_like(t_high)
            t_low[...] = jnp.zeros_like(t_low)
            for clip in range(2):
                for dh in range(2):
                    if clip == 0:
                        part = grad_ref[:, 2 * dh * width : (2 * dh + 1) * width]
                    else:
                        part = near_ref[:, dh * width : (dh + 1) * width]
                    high, low = split(part.T)
                    at = (slice(dh * width, (dh + 1) * width), slice(clip * padded, clip * padded + frames))
                    t_high[at] = high
                    t_low[at] = low
            for group in range(8):
                first, second, dh = group // 4, group // 2 % 2, group % 2
                core = place_ref[6]
                y = place_ref[4] ^ (first * core + second * (1 - core))
                x = place_ref[5] ^ (first * (1 - core) + second * core)
                at = pl.multiple_of(dh * width + (2 * y + x) * rows, rows)
                g_high[group * rows : (group + 1) * rows, :] = t_high[pl.ds(at, rows), :]
                g_low[group * rows : (group + 1) * rows, :] = t_low[pl.ds(at, rows), :]

    else:
        g_high, g_low, x_high, x_low, sent = refs
    half = g_high.shape[0] // 2
    value = product(g_high[half:, :], g_low[half:, :], x_high[...], x_low[...])
    sent[...] = value.reshape(sent.shape)


def leaving_rows(half, place, grads, x_split, width):
    turn = half == 0
    whole = lambda array: pl.BlockSpec(array.shape, lambda s, place: (0,) * array.ndim)
    x_spec = pl.BlockSpec((x_split[0].shape[0], width), lambda s, place: (0, 4 * half + s))
    shape = (2, 2, width // 4, 4 * width)
    out_shape = [jax.ShapeDtypeStruct(shape, F32)]
    out_specs = [pl.BlockSpec(shape[:3] + (width,), lambda s, place: (0, 0, 0, s))]
    scratch = []
    if turn:
        turned = (2 * width, x_split[0].shape[0])
        out_shape += [jax.ShapeDtypeStruct(turned, BF16)] * 2
        out_specs += [whole(out_shape[-1])] * 2
        scratch = [pltpu.VMEM(turned, BF16)] * 2
    return call(
        partial(leaving_body, turn),
        grid_spec=pltpu.PrefetchScalarGridSpec(
            num_scalar_prefetch=1,
            grid=(4,),
            in_specs=[whole(a) for a in grads] + [x_spec] * 2,
            out_specs=out_specs,
            scratch_shapes=scratch,
        ),
        out_shape=out_shape,
        cost_estimate=cost(6 * x_split[0].shape[0] * width * 4 * width, 4 * 4 * width * width),
        name="leaving_rows",
    )(place, *grads, *x_split)


def staying_body(g_high, g_low, x_high, x_low, kept):
    half = g_high.shape[0] // 2
    value = product(g_high[:half, :], g_low[:half, :], x_high[...], x_low[...])
    kept[...] = value.reshape(kept.shape)


def staying_rows(turned, x_split, width):
    whole = lambda array: pl.BlockSpec(array.shape, lambda s: (0,) * array.ndim)
    x_spec = pl.BlockSpec((x_split[0].shape[0], width), lambda s: (0, s))
    shape = (2, 2, width // 4, 8 * width)
    return call(
        staying_body,
        grid=(8,),
        in_specs=[whole(a) for a in turned] + [x_spec] * 2,
        out_specs=pl.BlockSpec(shape[:3] + (width,), lambda s: (0, 0, 0, s)),
        out_shape=jax.ShapeDtypeStruct(shape, F32),
        cost_estimate=cost(6 * x_split[0].shape[0] * width * 8 * width, 4 * 8 * width * width),
        name="staying_rows",
    )(*turned, *x_split)


def plane_swap(array, step):
    pairs = []
    for i in range(8):
        over_x = (i % 2 == 0) == (step == 0)
        pairs.append((i, i ^ 2 if over_x else i ^ 4))
    return lax.ppermute(array, ("y", "x", "c"), pairs)


def plane_gather(share):
    first = plane_swap(share, 0)
    second = plane_swap(share, 1)
    return [share, second, first, plane_swap(first, 1)]


def assemble_body(groups, place_ref, *refs):
    out_ref = refs[-1]
    core = place_ref[6]
    column = 0
    for group in range(groups):
        rows, columns = refs[4 * group].shape
        for i in range(4):
            first, second = i // 2, i % 2
            y = place_ref[4] ^ (first * core + second * (1 - core))
            x = place_ref[5] ^ (first * (1 - core) + second * core)
            at = pl.multiple_of((2 * y + x) * rows, rows)
            out_ref[..., pl.ds(at, rows), column : column + columns] = refs[4 * group + i][
                ...
            ].reshape(out_ref.shape[:-2] + (rows, columns))
        column += columns


def assemble(place, groups, layer=None, onto=None):
    pieces = [piece for group in groups for piece in group]
    rows = pieces[0].shape[0]
    shape = (4 * rows, sum(group[0].shape[1] for group in groups))
    out_spec = pl.BlockSpec(shape, lambda i: (0, 0))
    aliases, extra, extra_specs = {}, [], []
    if layer is not None:
        out_spec = pl.BlockSpec((1, *shape), lambda i: (layer, 0, 0))
        aliases, extra = {1 + len(pieces): 0}, [onto]
        extra_specs = [pl.BlockSpec(memory_space=pl.ANY)]
        shape = (LAYERS, *shape)
    return call(
        partial(assemble_body, len(groups)),
        grid=(1,),
        out_shape=jax.ShapeDtypeStruct(shape, F32),
        in_specs=[SMEM_SPEC]
        + [pl.BlockSpec(p.shape, lambda i: (0, 0)) for p in pieces]
        + extra_specs,
        out_specs=out_spec,
        input_output_aliases=aliases,
        cost_estimate=cost(0, 8 * shape[-1] * shape[-2]),
        name="assemble",
    )(place, *pieces, *extra)


def keep_body(in_ref, out_ref):
    out_ref[0] = in_ref[...]


def keep(array, layer):
    return call(
        keep_body,
        grid=(1,),
        out_shape=jax.ShapeDtypeStruct((LAYERS, *array.shape), F32),
        in_specs=[pl.BlockSpec(array.shape, lambda i: (0, 0))],
        out_specs=pl.BlockSpec((1, *array.shape), lambda i: (layer, 0, 0)),
        cost_estimate=cost(0, 8 * array.size),
        name="keep",
    )(array)


def after(value, *others):
    return lax.optimization_barrier((value, others))[0]


def half_features(inputs, weights, gains, shifts, decays, biases, lengths, frame_mask, grad_out):
    width, slots = inputs.shape
    clips, frames = frame_mask.shape
    depth = weights.shape[2]
    blocks = 4 * width // LANES
    y, x, h, l, c = (lax.axis_index(name) for name in ("y", "x", "h", "l", "c"))
    b = 2 * y + x
    numbers = [2 * (h ^ (rel // 2)) + (c ^ (rel % 2)) for rel in range(4)] + [y, x, c]
    place = jnp.stack(numbers).astype(jnp.int32)
    own_blocks, other_blocks = (
        jnp.stack(
            [2 * (2 * (h ^ (rel // 2)) + half) + (c ^ (rel % 2)) for rel in range(4)]
        ).astype(jnp.int32)
        for half in (l, 1 - l)
    )
    all_blocks = jnp.concatenate([own_blocks, other_blocks])
    own_columns = jnp.stack([2 * h + l, 2 * (1 - h) + l]).astype(jnp.int32)
    other_columns = jnp.stack([2 * (1 - h) + 1 - l, 2 * h + 1 - l]).astype(jnp.int32)
    rows = width // 4

    clip = 2 * h + c
    seen = lax.dynamic_index_in_dim(frame_mask, clip, 0, keepdims=False)
    length = lax.dynamic_index_in_dim(lengths, clip, 0, keepdims=False)
    moments = jnp.arange(frames, dtype=jnp.int32)
    gate = ((moments < length) & ((seen == 1) | (moments == 0))).astype(F32)
    valid = jnp.broadcast_to(gate[:, None], (frames, LANES))

    def far_share(layer):
        return lax.dynamic_slice(weights, (layer, b * rows, 0), (1, rows, depth))[0]

    def over_h(array):
        return lax.ppermute(array, "h", FLIP2)

    def over_c(array):
        return lax.ppermute(array, "c", FLIP2)

    def over_second(array):
        return plane_swap(array, 1)

    def four_of(near_rows, far_rows):
        return [
            (near_rows, 0),
            (over_c(near_rows), 1),
            (far_rows, 0),
            (over_c(far_rows), 1),
        ]

    near = over_c(weights)
    share = far_share(0)
    close, away = pack(place, after(inputs, share), frames)
    share = over_h(share)
    other_close = swap_half(close)
    up_close, up_away = pack(place, after(grad_out, close), frames)
    params = jnp.stack([gains, shifts + biases, decays], axis=1).reshape(LAYERS, 3, width)
    gathered = lax.all_gather(after(params, up_close), ("h", "c"), axis=2, tiled=True)
    params = gathered.reshape(LAYERS, 3, blocks, LANES)
    share = after(share, gathered, valid)
    away = over_h(after(away, share, other_close))
    far = assemble(place, after([plane_gather(share)], away))
    own = four_of(close, away)
    others = four_of(other_close, swap_half(away))
    half_weights = [[weights, near, far, over_c(far)]]
    share = over_h(after(far_share(1), away))

    saved = []
    chunk_plan = (2, 1)
    for layer in range(LAYERS):
        last = layer == LAYERS - 1
        flat = layer == 0
        if layer > 0:
            others = [(swap_half(array), None) for array, _ in own]
        z, *own_flat = project(
            own_blocks, place, frames, own, half_weights[layer], layer, flat=flat
        )
        z, stats, *other_flat = project(
            other_blocks, place, frames, others, half_weights[layer], layer, z, valid, flat=flat
        )
        if last:
            upstream = four_of(up_close, over_h(after(up_away, z)))
        plane = lax.all_gather(stats, ("y", "x"))
        if not last:
            far = lax.all_gather(after(share, plane), ("y", "x"), axis=0, tiled=True)
            half_weights.append([weights, near, far, over_c(far)])
        stats = lax.all_gather(plane, ("h", "c")).reshape(16, *stats.shape)
        chunks = chunk_plan[layer]
        state = jnp.zeros((blocks, LANES), F32)
        following, states, slopes = [], [], []
        for chunk in range(chunks):
            *new, kept, slope, state = recur(
                chunk, chunks, place, gate, z, stats, params[layer], valid, state, own, last
            )
            following.extend(new)
            states.append(kept)
            slopes.append(slope)
        if flat:
            groups = [own_flat, other_flat]
        else:
            groups = [arrays_of(own), arrays_of(others)]
        groups += [[over_c(after(p, state)) for p in group] for group in groups]
        x_split = prepare(all_blocks, groups) if flat else None
        saved.append((groups, x_split, z, stats, states, slopes))
        own = [(array, None) for array in following]
    close, away = following
    away = over_h(away)
    output = four_of(close, away)

    ups = upstream
    results = [None] * LAYERS
    for layer in range(LAYERS - 1, -1, -1):
        groups, x_split, z, stats, states, slopes = saved[layer]
        weight = half_weights[layer]
        grad_pre, sums = back(place, gate, z, stats, params[layer], ups, states, slopes)
        plane = lax.all_gather(sums, ("y", "x"))
        if layer == 0:
            total = [k + after(g, plane) for k, g in zip(stay, come)]
            plane = after(plane, total)
            come = over_second(jnp.concatenate([t[1] for t in total], axis=-1))
        sums = lax.all_gather(plane, ("h", "c")).reshape(16, *sums.shape)
        grad_z, leaving, *terms, sums = norm_back(
            other_columns, place, grad_pre, z, params[layer], valid, stats, sums, weight, layer,
            layer == 0,
        )
        leaving = over_c(leaving)
        if layer > 0:
            received = [swap_half(terms[0])]
            x_split = prepare(all_blocks, after(groups, grad_z, away))
        else:
            total = jnp.concatenate([t[0] for t in total], axis=-1) + after(come, grad_z)
            later = (total[0], over_h(total[1]))
            leaving = after(leaving, later[0])
            received = [None, swap_half(terms[1])]
        sent, *g_split = leaving_rows(0, place, (grad_z, leaving), x_split, width)
        come = [plane_swap(sent, 0)]
        if layer == 0:
            g_split = after(g_split, received[1])
            received[0] = swap_half(after(terms[0], received[1]))
        (sent,) = leaving_rows(1, place, g_split, x_split, width)
        come.append(plane_swap(sent, 0))
        kept = own_terms(own_columns, place, after(grad_z, sent), ups, weight, layer)
        half = depth // 2
        if layer > 0:
            stay = staying_rows(after(g_split, kept), x_split, width)
            stay = (stay[..., :half], stay[..., half:])
            ups = [(kept, None)] + [(r, None) for r in received]
        results[layer] = lax.dynamic_index_in_dim(
            sums.reshape(3, 4, width), clip, axis=1, keepdims=False
        )

    away = merge(kept, 1, received[1])
    stay = staying_rows(after(g_split, away), x_split, width)
    away = over_h(away)
    stay = (stay[..., :half], stay[..., half:])
    first = stay[0] + come[0]
    second = stay[1] + after(come[1], first)
    come = [over_second(first[1]), over_second(second[1])]
    close = merge(kept, 0, after(received[0], second))
    first = first[0] + after(come[0], close)
    second = second[0] + after(come[1], first)
    come = [over_h(first[1]), over_h(second[1])]
    later = later[0] + after(later[1], second)
    later = lax.all_gather(later, ("y", "x"), axis=0, tiled=True)
    output = [(after(array, second), i) for array, i in output]
    output = unpack(place, output, frames)
    first = first[0] + after(come[0], output)
    second = second[0] + after(come[1], first)
    gathered = [plane_gather(first), plane_gather(second)]
    grad_in = [(after(array, second), i) for array, i in four_of(close, away)]
    grad_in = unpack(place, grad_in, frames)
    grad_weights = keep(after(later, grad_in), 1)
    grad_weights = assemble(place, gathered, 0, grad_weights)
    sums = jnp.stack(results)
    return (
        output,
        grad_in,
        grad_weights,
        sums[:, 0],
        sums[:, 1],
        sums[:, 2],
        sums[:, 1],
    )


def gelu_slope(value):
    return (
        0.5 * (1.0 + jax.scipy.special.erf(value / ROOT_TWO))
        + value * jnp.exp(-0.5 * value * value) / ROOT_TWO_PI
    )


def recur_step(decay, state, inputs):
    drive_t, valid_t = inputs
    pre = drive_t + decay * state
    state = state + valid_t * (jax.nn.gelu(pre, approximate=False) - state)
    return (state, state)


def back_step(decay, carry, inputs):
    upstream_t, valid_t, pre_t = inputs
    total = upstream_t + carry
    grad_pre = total * valid_t * gelu_slope(pre_t)
    carry = total * (1.0 - valid_t) + grad_pre * decay
    return (carry, grad_pre)


def add_piece(weight, piece):
    return jnp.dot(weight, piece, precision=HIGH, preferred_element_type=jnp.float32)


def weight_columns(grad_pre_norm, piece):
    return jnp.einsum("jf,kf->jk", grad_pre_norm, piece, precision=HIGH)


def split_features(inputs, weights, gains, shifts, decays, biases, lengths, frame_mask, grad_out):
    width, slots = inputs.shape
    clips, frames_len = frame_mask.shape
    frames = jnp.arange(frames_len, dtype=jnp.int32)
    valid_grid = (
        (frames[None, :] < lengths[:, None]) & ((frame_mask == 1) | (frames[None, :] == 0))
    ).astype(jnp.float32)
    valid = valid_grid.reshape(-1)
    valid_row = valid[None, :]
    valid_time = jnp.broadcast_to(valid_grid.T[:, :, None], (frames_len, clips, width)).reshape(
        frames_len, clips * width
    )
    count_local = jnp.sum(valid)

    def to_time(array):
        return jnp.transpose(array.reshape(width, clips, frames_len), (2, 1, 0)).reshape(
            frames_len, clips * width
        )

    def from_time(array):
        return jnp.transpose(array.reshape(frames_len, clips, width), (2, 1, 0)).reshape(
            width, slots
        )

    layer_in = inputs
    saved = []
    for layer_no in range(LAYERS):
        weight = weights[layer_no]
        gathered = lax.all_gather(layer_in, "neuron", axis=0, tiled=True)
        pre_norm = add_piece(weight, gathered)
        first_sum, count = lax.psum((jnp.sum(valid_row * pre_norm, axis=1), count_local), "batch")
        mean = first_sum / count
        centered = pre_norm - mean[:, None]
        var = lax.psum(jnp.sum(valid_row * centered * centered, axis=1), "batch") / count
        inv_std = lax.rsqrt(var + EPS)
        zhat = (pre_norm - mean[:, None]) * inv_std[:, None]
        drive = gains[layer_no][:, None] * zhat + (shifts[layer_no] + biases[layer_no])[:, None]
        drive_time = to_time(drive)
        decay_wide = jnp.tile(decays[layer_no], clips)
        start_state = jnp.zeros((clips * width,), jnp.float32)
        _, states = lax.scan(
            partial(recur_step, decay_wide), start_state, (drive_time, valid_time), unroll=8
        )
        saved.append((gathered, zhat, inv_std, drive_time, states, count))
        layer_in = layer_in + valid_row * from_time(states)
    upstream = grad_out
    grad_parts = [None] * LAYERS
    for layer_no in range(LAYERS - 1, -1, -1):
        gathered, zhat, inv_std, drive_time, states, count = saved[layer_no]
        decay_wide = jnp.tile(decays[layer_no], clips)
        gain = gains[layer_no]
        previous = jnp.concatenate([jnp.zeros_like(states[:1]), states[:-1]], axis=0)
        pre_time = drive_time + decay_wide[None, :] * previous
        grad_state = to_time(valid_row * upstream)
        start_carry = jnp.zeros((clips * width,), jnp.float32)
        _, grad_pre_time = lax.scan(
            partial(back_step, decay_wide),
            start_carry,
            (grad_state, valid_time, pre_time),
            reverse=True,
            unroll=8,
        )
        decay_local = jnp.sum(
            jnp.sum(grad_pre_time * previous, axis=0).reshape(clips, width), axis=0
        )
        grad_pre = from_time(grad_pre_time)
        gain_local = jnp.sum(grad_pre * zhat, axis=1)
        shift_local = jnp.sum(grad_pre, axis=1)
        grad_gain, grad_shift, grad_decay = lax.psum(
            (gain_local, shift_local, decay_local), "batch"
        )
        grad_pre_norm = (gain * inv_std)[:, None] * (
            grad_pre - valid_row * (grad_shift[:, None] + zhat * grad_gain[:, None]) / count
        )
        weight_local = weight_columns(grad_pre_norm, gathered)
        input_terms = jnp.einsum("jk,jf->kf", weights[layer_no], grad_pre_norm, precision=HIGH)
        input_grad = lax.psum_scatter(input_terms, "neuron", scatter_dimension=0, tiled=True)
        grad_weight = lax.psum(weight_local, "batch")
        upstream = upstream + input_grad
        grad_parts[layer_no] = (grad_weight, grad_gain, grad_shift, grad_decay)
    grad_weights = jnp.stack([grad_parts[layer_no][0] for layer_no in range(LAYERS)])
    grad_gains = jnp.stack([grad_parts[layer_no][1] for layer_no in range(LAYERS)])
    grad_shifts = jnp.stack([grad_parts[layer_no][2] for layer_no in range(LAYERS)])
    grad_decays = jnp.stack([grad_parts[layer_no][3] for layer_no in range(LAYERS)])
    return (layer_in, upstream, grad_weights, grad_gains, grad_shifts, grad_decays, grad_shifts)


def solution(mesh):
    if (mesh.shape["batch"], mesh.shape["neuron"]) == (4, 8):
        cut = Mesh(mesh.devices.reshape(2, 2, 2, 2, 2), ("y", "x", "h", "l", "c"))
        batch, neuron, body = ("y", "x"), ("h", "l", "c"), half_features
    else:
        cut, batch, neuron, body = mesh, "batch", "neuron", split_features
    in_specs = (
        P(neuron, batch),
        P(None, neuron, None),
        P(None, neuron),
        P(None, neuron),
        P(None, neuron),
        P(None, neuron),
        P(batch),
        P(batch, None),
        P(neuron, batch),
    )
    out_specs = (
        P(neuron, batch),
        P(neuron, batch),
        P(None, neuron, None),
        P(None, neuron),
        P(None, neuron),
        P(None, neuron),
        P(None, neuron),
    )
    return jax.shard_map(
        body, mesh=cut, in_specs=in_specs, out_specs=out_specs, check_vma=False
    )
```

```python
from functools import partial
import math

import jax
import jax.numpy as jnp
from jax import lax
from jax.experimental import pallas as pl
from jax.experimental.pallas import tpu as pltpu
from jax.sharding import Mesh, PartitionSpec as P

LAYERS = 2
EPS = 1e-05
HIGH = lax.Precision.HIGHEST
ROOT_TWO = math.sqrt(2.0)
ROOT_TWO_PI = math.sqrt(2.0 * math.pi)
F32 = jnp.float32
BF16 = jnp.bfloat16
LANES = 128
VMEM_LIMIT = 24 * 1024 * 1024
SMEM_SPEC = pl.BlockSpec(memory_space=pltpu.SMEM)
VMEM_SPEC = pl.BlockSpec(memory_space=pltpu.VMEM)


FLIP2 = [(0, 1), (1, 0)]


def swap_half(array):
    return lax.ppermute(array, "l", FLIP2)


def after(value, *others):
    return lax.optimization_barrier((value, others))[0]


def split(value):
    high = value.astype(BF16)
    return high, (value - high.astype(F32)).astype(BF16)


def dot(a, b, dims):
    return lax.dot_general(a, b, (dims, ((), ())), preferred_element_type=F32)


NT = ((1,), (1,))
NN = ((1,), (0,))


def call(body, **kwargs):
    return pl.pallas_call(
        body,
        compiler_params=pltpu.CompilerParams(vmem_limit_bytes=VMEM_LIMIT),
        **kwargs,
    )


def cost(flops, byte_count):
    return pl.CostEstimate(flops=int(flops) // 64, bytes_accessed=int(byte_count) // 64, transcendentals=0)


def pack_body(frames, place_ref, in_ref, near_ref, far_ref, turned):
    slots = in_ref.shape[1]
    for start in range(0, slots, LANES):
        turned[start : start + LANES, :] = in_ref[:, start : start + LANES].T
    for rel in range(4):
        first = pl.multiple_of(place_ref[rel] * frames, 8)
        out = (near_ref, far_ref)[rel // 2]
        out[(rel % 2) * frames : (rel % 2 + 1) * frames, :] = turned[pl.ds(first, frames), :]


def pack(place, array, frames):
    width, slots = array.shape
    return call(
        partial(pack_body, frames),
        out_shape=[jax.ShapeDtypeStruct((2 * frames, width), F32)] * 2,
        in_specs=[SMEM_SPEC, VMEM_SPEC],
        out_specs=[VMEM_SPEC] * 2,
        scratch_shapes=[pltpu.VMEM((slots, width), F32)],
        cost_estimate=cost(0, 8 * width * slots),
        name="pack",
    )(place, array)


def part_spec(part, frames):
    array, i = part
    if i is None:
        return pl.BlockSpec(array.shape, lambda *_: (0,) * array.ndim)
    return pl.BlockSpec((frames, array.shape[1]), lambda *_: (i, 0))


def arrays_of(parts):
    return [array for array, _ in parts]


def unpack_body(frames, place_ref, *refs):
    ins, out_ref, turned = refs[:4], refs[4], refs[5]
    slots = out_ref.shape[1]
    for rel in range(4):
        first = pl.multiple_of(place_ref[rel] * frames, 8)
        turned[pl.ds(first, frames), :] = ins[rel][...]
    for start in range(0, slots, LANES):
        out_ref[:, start : start + LANES] = turned[start : start + LANES, :].T


def unpack(place, parts, frames):
    width = parts[0][0].shape[1]
    slots = 4 * frames
    return call(
        partial(unpack_body, frames),
        grid=(1,),
        out_shape=jax.ShapeDtypeStruct((width, slots), F32),
        in_specs=[SMEM_SPEC] + [part_spec(part, frames) for part in parts],
        out_specs=pl.BlockSpec((width, slots), lambda i: (0, 0)),
        scratch_shapes=[pltpu.VMEM((slots, width), F32)],
        cost_estimate=cost(0, 8 * width * slots),
        name="unpack",
    )(place, *arrays_of(parts))


def merge_body(kept_ref, come_ref, out_ref):
    frames, columns = kept_ref.shape
    width = columns // 2
    for i in range(2):
        some = slice(i * width, (i + 1) * width)
        out_ref[i * frames : (i + 1) * frames, :] = kept_ref[:, some] + come_ref[:, some]


def merge(kept, half, come):
    frames, columns = come.shape
    return call(
        merge_body,
        grid=(1,),
        out_shape=jax.ShapeDtypeStruct((2 * frames, columns // 2), F32),
        in_specs=[
            pl.BlockSpec((frames, columns), lambda i: (0, half)),
            pl.BlockSpec((frames, columns), lambda i: (0, 0)),
        ],
        out_specs=pl.BlockSpec((2 * frames, columns // 2), lambda i: (0, 0)),
        cost_estimate=cost(0, 12 * frames * columns),
        name="merge",
    )(kept, come)


def spread_of(parts, width):
    spots, row, column = [], 0, 0
    for array, _ in parts:
        spots.append((row, column))
        if array.shape[1] == width:
            column += width
        else:
            row += array.shape[0]
    return spots


def project_body(n_parts, spots, with_acc, with_stats, flat, cols_ref, place_ref, *refs):
    del cols_ref
    parts, refs = refs[:n_parts], refs[n_parts:]
    weights, refs = refs[:4], refs[4:]
    if with_acc:
        acc_ref, refs = refs[0], refs[1:]
    if with_stats:
        valid_ref, refs = refs[0], refs[1:]
    out_ref, refs = refs[0], refs[1:]
    if with_stats:
        stats_ref, refs = refs[0], refs[1:]
    if flat:
        flat_ref, refs = refs[0], refs[1:]
    x_high, x_low = refs
    step = pl.program_id(0)
    width = x_high.shape[2]

    @pl.when(step == 0)
    def _():
        for (row, column), part in zip(spots, parts):
            rows, columns = part.shape
            for start in range(0, columns, width):
                rel = (column + start) // width
                high, low = split(part[:, start : start + width])
                x_high[rel, row : row + rows, :] = high
                x_low[rel, row : row + rows, :] = low
            if flat:
                flat_ref[row : row + rows, column : column + columns] = part[...]
        if with_acc:
            out_ref[...] = acc_ref[...]
        else:
            out_ref[...] = jnp.zeros_like(out_ref)

    stacked = jnp.concatenate([x_high[step], x_low[step], x_high[step]], axis=1)
    for block in range(4):
        w_high, w_low = split(weights[block][...].reshape(width, width))
        columns = slice(block * width, (block + 1) * width)
        out_ref[:, columns] += dot(stacked, jnp.concatenate([w_high, w_high, w_low], axis=1), NT)

    if with_stats:

        @pl.when(step == pl.num_programs(0) - 1)
        def _():
            valid = valid_ref[...]
            own = jnp.sum(valid, axis=0, keepdims=True)
            per = width // LANES
            for row in range(out_ref.shape[1] // LANES):
                z = out_ref[:, row * LANES : (row + 1) * LANES]
                total = jnp.sum(valid * z, axis=0, keepdims=True)
                centred = valid * (z - total / own)
                squares = jnp.sum(centred * centred, axis=0, keepdims=True)
                at = place_ref[row // per] * per + row % per
                stats_ref[0, pl.ds(at, 1), :] = total
                stats_ref[1, pl.ds(at, 1), :] = squares
                stats_ref[2, pl.ds(at, 1), :] = own


def weight_specs(weights, layer, pairs=2):
    specs = []
    for weight in weights:
        width = weight.shape[-2]
        if weight.ndim == 3:
            specs.append(
                pl.BlockSpec((1, width, pairs * width), lambda s, cols, *_: (layer, 0, cols[s]))
            )
        else:
            specs.append(pl.BlockSpec((width, pairs * width), lambda s, cols, *_: (0, cols[s])))
    return specs


def project(columns, place, frames, parts, weights, layer, acc=None, valid=None, flat=False):
    width = weights[0].shape[-2]
    full = pl.BlockSpec(memory_space=pltpu.VMEM)
    in_specs = [part_spec(part, frames) for part in parts]
    in_specs += weight_specs(weights, layer, 1)
    operands = arrays_of(parts) + list(weights)
    array = jax.ShapeDtypeStruct((frames, 4 * width), F32)
    array_spec = pl.BlockSpec((frames, 4 * width), lambda s, cols, place: (0, 0))
    out_shape, out_specs = [array], [array_spec]
    if acc is not None:
        in_specs.append(full)
        operands.append(acc)
    if valid is not None:
        in_specs.append(full)
        operands.append(valid)
        rows = 4 * width // LANES
        out_shape.append(jax.ShapeDtypeStruct((3, rows, LANES), F32))
        out_specs.append(pl.BlockSpec((3, rows, LANES), lambda s, cols, place: (0, 0, 0)))
    if flat:
        out_shape.append(array)
        out_specs.append(array_spec)
    return call(
        partial(
            project_body,
            len(parts),
            spread_of(parts, width),
            acc is not None,
            valid is not None,
            flat,
        ),
        grid_spec=pltpu.PrefetchScalarGridSpec(
            num_scalar_prefetch=2,
            grid=(4,),
            in_specs=in_specs,
            out_specs=out_specs,
            scratch_shapes=[pltpu.VMEM((4, frames, width), BF16)] * 2,
        ),
        out_shape=out_shape,
        cost_estimate=cost(2 * 3 * frames * 16 * width * width, 4 * 16 * width * width),
        name="project",
    )(columns, place, *operands)


def to_relative(place_ref, spread, rows_ref, value, slot):
    per = value.shape[0] // 4
    spread[...] = value
    for rel in range(4):
        first = place_ref[rel] * per
        for row in range(per):
            rows_ref[slot, rel * per + row : rel * per + row + 1, :] = spread[
                pl.ds(first + row, 1), :
            ]


def tree(values):
    while len(values) > 1:
        values = [a + b for a, b in zip(values[::2], values[1::2])]
    return values[0]


def norm_terms(stats_ref):
    each = [[stats_ref[i] for i in range(slot, stats_ref.shape[0], 3)] for slot in range(3)]
    totals, squares, owns = each
    count = tree(owns)
    mean = tree(totals) / count
    away = [total / own - mean for total, own in zip(totals, owns)]
    spread = tree([s + n * a * a for s, n, a in zip(squares, owns, away)])
    return count, mean, lax.rsqrt(spread / count + EPS)


def recur_body(n_parts, spots, n_out, first, place_ref, gate_ref, z_ref, stats_ref, params_ref, valid_ref, start_ref, *refs):
    parts, refs = refs[:n_parts], refs[n_parts:]
    outs, refs = refs[:n_out], refs[n_out:]
    state_ref, slope_ref, last_ref, rows, spread, drive_s, state_s, slope_s = refs
    frames = z_ref.shape[0]
    blocks = z_ref.shape[1] // LANES
    _, mean, inv_std = norm_terms(stats_ref)
    to_relative(place_ref, spread, rows, mean, 0)
    to_relative(place_ref, spread, rows, params_ref[0] * inv_std, 1)
    to_relative(place_ref, spread, rows, params_ref[1], 2)
    to_relative(place_ref, spread, rows, params_ref[2], 3)
    for row in range(blocks):
        z = z_ref[:, row * LANES : (row + 1) * LANES]
        drive_s[row * frames : (row + 1) * frames, :] = (
            z - rows[0, row : row + 1, :]
        ) * rows[1, row : row + 1, :] + rows[2, row : row + 1, :]
    decay = rows[3]

    def step(t, state):
        at = pl.ds(t, blocks, stride=frames)
        pre = drive_s[at, :] + decay * state
        half = 0.5 + 0.5 * lax.erf(pre * (1.0 / ROOT_TWO))
        gate = gate_ref[first + t] > 0.0
        slope = half + pre * jnp.exp(-0.5 * pre * pre) * (1.0 / ROOT_TWO_PI)
        state = jnp.where(gate, pre * half, state)
        state_s[at, :] = state
        slope_s[at, :] = jnp.where(gate, slope, 0.0)
        return state

    last_ref[...] = lax.fori_loop(0, frames, step, start_ref[...], unroll=8)
    valid = valid_ref[...]
    for row in range(blocks):
        lanes = slice(row * LANES, (row + 1) * LANES)
        state = state_s[row * frames : (row + 1) * frames, :]
        state_ref[:, lanes] = state
        slope_ref[:, lanes] = slope_s[row * frames : (row + 1) * frames, :]
        for (top, column), part in zip(spots, parts):
            if column <= row * LANES < column + part.shape[1]:
                x = part[:, row * LANES - column : (row + 1) * LANES - column]
                some = slice(top, top + part.shape[0])
                out, base, at = outs[0], top, row * LANES
                if len(outs) > 1:
                    rel, inner = divmod(row * LANES, outs[0].shape[1])
                    out, base, at = outs[rel // 2], (rel % 2) * frames + top, inner
                out[base : base + part.shape[0], at : at + LANES] = x + valid[some] * state[some]


def recur(chunk, chunks, place, gate, z, stats, params, valid, start, parts, last):
    frames = z.shape[0] // chunks
    features = z.shape[1]
    width = features // 4
    blocks = features // LANES
    row_block = lambda columns: pl.BlockSpec((frames, columns), lambda i: (chunk, 0))
    whole = lambda array: pl.BlockSpec(array.shape, lambda i: (0,) * array.ndim)
    part_specs = []
    for array, at in parts:
        if at is None:
            part_specs.append(whole(array))
        else:
            part_specs.append(
                pl.BlockSpec((frames, width), lambda i, at=at: (at * chunks + chunk, 0))
            )
    tile = jax.ShapeDtypeStruct((blocks, LANES), F32)
    full = jax.ShapeDtypeStruct((frames, features), F32)
    outs = [jax.ShapeDtypeStruct((2 * frames, width), F32)] * 2 if last else [full]
    out_shape = outs + [full, full, tile]
    return call(
        partial(recur_body, len(parts), spread_of(parts, width), len(outs), chunk * frames),
        grid=(1,),
        in_specs=[
            SMEM_SPEC,
            SMEM_SPEC,
            row_block(features),
            whole(stats),
            whole(params),
            row_block(LANES),
            whole(start),
        ]
        + part_specs,
        out_specs=[whole(s) for s in out_shape],
        out_shape=out_shape,
        scratch_shapes=[
            pltpu.VMEM((4, blocks, LANES), F32),
            pltpu.VMEM((blocks, LANES), F32),
        ]
        + [pltpu.VMEM((blocks * frames, LANES), F32)] * 3,
        cost_estimate=cost(100 * frames * features, 20 * frames * features),
        name="recur",
    )(place, gate, z, stats, params, valid, start, *arrays_of(parts))


def back_body(n_parts, spots, n_state, place_ref, gate_ref, z_ref, stats_ref, params_ref, *refs):
    parts, refs = refs[:n_parts], refs[n_parts:]
    states, refs = refs[:n_state], refs[n_state:]
    slopes, refs = refs[:n_state], refs[n_state:]
    grad_ref, sums_ref, rows, spread, up_s, state_s, slope_s = refs
    frames = z_ref.shape[0]
    blocks = z_ref.shape[1] // LANES
    tall = frames + 8
    _, mean, inv_std = norm_terms(stats_ref)
    to_relative(place_ref, spread, rows, mean, 0)
    to_relative(place_ref, spread, rows, inv_std, 1)
    to_relative(place_ref, spread, rows, params_ref[2], 2)
    for row in range(blocks):
        lanes = slice(row * LANES, (row + 1) * LANES)
        base = row * frames
        up = None
        for (top, column), part in zip(spots, parts):
            if column <= row * LANES < column + part.shape[1] and part.shape[0] == frames:
                value = part[:, row * LANES - column : (row + 1) * LANES - column]
                up = value if up is None else up + value
        up_s[base : base + frames, :] = up
        state_s[row * tall : row * tall + 8, :] = jnp.zeros((8, LANES), F32)
        first = 0
        for state, slope in zip(states, slopes):
            some = state.shape[0]
            at = row * tall + 8 + first
            state_s[at : at + some, :] = state[:, lanes]
            slope_s[base + first : base + first + some, :] = slope[:, lanes]
            first += some
    decay = rows[2]

    def step(i, carry):
        t = frames - 1 - i
        at = pl.ds(t, blocks, stride=frames)
        slope = slope_s[at, :]
        gate = gate_ref[t]
        total = gate * up_s[at, :] + carry
        up_s[at, :] = total * slope
        return total * (slope * decay + (1.0 - gate))

    lax.fori_loop(0, frames, step, jnp.zeros((blocks, LANES), F32), unroll=8)
    per = blocks // 4
    for row in range(blocks):
        lanes = slice(row * LANES, (row + 1) * LANES)
        base = row * frames
        grad = up_s[base : base + frames, :]
        grad_ref[:, lanes] = grad
        zhat = (z_ref[:, lanes] - rows[0, row : row + 1, :]) * rows[1, row : row + 1, :]
        before = state_s[row * tall + 7 : row * tall + 7 + frames, :]
        at = place_ref[row // per] * per + row % per
        for slot, value in enumerate((grad * zhat, grad, grad * before)):
            sums_ref[slot, pl.ds(at, 1), :] = jnp.sum(value, axis=0, keepdims=True)


def spots_of_sum(parts, width):
    spots, column = [], 0
    for array, _ in parts:
        spots.append((0, column % (4 * width)))
        column += array.shape[1]
    return spots


def back(place, gate, z, stats, params, ups, states, slopes):
    frames, features = z.shape
    width = features // 4
    blocks = features // LANES
    whole = lambda array: pl.BlockSpec(array.shape, lambda i: (0,) * array.ndim)
    out_shape = [
        jax.ShapeDtypeStruct((frames, features), F32),
        jax.ShapeDtypeStruct((3, blocks, LANES), F32),
    ]
    return call(
        partial(back_body, len(ups), spots_of_sum(ups, width), len(states)),
        grid=(1,),
        in_specs=[SMEM_SPEC] * 2
        + [whole(a) for a in (z, stats, params)]
        + [part_spec(up, frames) for up in ups]
        + [whole(a) for a in (*states, *slopes)],
        out_specs=[whole(a) for a in out_shape],
        out_shape=out_shape,
        scratch_shapes=[
            pltpu.VMEM((3, blocks, LANES), F32),
            pltpu.VMEM((blocks, LANES), F32),
            pltpu.VMEM((blocks * frames, LANES), F32),
            pltpu.VMEM((blocks * (frames + 8), LANES), F32),
            pltpu.VMEM((blocks * frames, LANES), F32),
        ],
        cost_estimate=cost(30 * frames * features, 20 * frames * features),
        name="back",
    )(place, gate, z, stats, params, *arrays_of(ups), *states, *slopes)


def input_terms(high_s, low_s, weights):
    width = high_s.shape[2]
    left, right = [], []
    for block, weight in enumerate(weights):
        w_high, w_low = split(weight[...].reshape(width, 2 * width))
        left += [high_s[block], low_s[block], high_s[block]]
        right += [w_high, w_high, w_low]
    return dot(jnp.concatenate(left, axis=1), jnp.concatenate(right, axis=0), NN)


def norm_back_body(split_terms, cols_ref, place_ref, grad_ref, z_ref, params_ref, valid_ref, stats_ref, sums_ref, *refs):
    del cols_ref
    weights, refs = refs[:4], refs[4:]
    if split_terms:
        out_ref, leave_ref, near_term_ref, far_term_ref, sums_out_ref, *refs = refs
        term_refs, starts = (far_term_ref, near_term_ref), (0, 0)
    else:
        out_ref, leave_ref, term_ref, sums_out_ref, *refs = refs
        term_refs, starts = (term_ref, term_ref), (2 * grad_ref.shape[1] // 4, 0)
    rows, spread, high_s, low_s = refs
    blocks = z_ref.shape[1] // LANES
    width = high_s.shape[2]
    per = width // LANES

    @pl.when(pl.program_id(0) == 0)
    def _():
        count, mean, inv_std = norm_terms(stats_ref)
        to_relative(place_ref, spread, rows, mean, 0)
        to_relative(place_ref, spread, rows, inv_std, 1)
        to_relative(place_ref, spread, rows, params_ref[0] * inv_std, 2)
        sums = tree([sums_ref[i : i + 3] for i in range(0, sums_ref.shape[0], 3)])
        sums_out_ref[...] = sums
        to_relative(place_ref, spread, rows, sums[0] / count, 3)
        to_relative(place_ref, spread, rows, sums[1] / count, 4)
        valid = valid_ref[...]
        for row in range(blocks):
            lanes = slice(row * LANES, (row + 1) * LANES)
            one = lambda slot: rows[slot, row : row + 1, :]
            zhat = (z_ref[:, lanes] - one(0)) * one(1)
            value = one(2) * (grad_ref[:, lanes] - valid * (one(4) + zhat * one(3)))
            out_ref[:, lanes] = value
            if (row // per) % 2:
                at = (row // per // 2) * width + (row % per) * LANES
                leave_ref[:, at : at + LANES] = value
            high, low = split(value)
            inner = slice((row % per) * LANES, (row % per + 1) * LANES)
            high_s[row // per, :, inner] = high
            low_s[row // per, :, inner] = low

    value = input_terms(high_s, low_s, weights)
    for step, (term_ref, first) in enumerate(zip(term_refs, starts)):

        @pl.when(pl.program_id(0) == step)
        def _():
            for pair in range(2):
                at = pl.multiple_of(((place_ref[0] & 1) ^ pair) * width, width)
                term_ref[:, pl.ds(first + at, width)] = value[
                    :, pair * width : (pair + 1) * width
                ]


def norm_back(columns, place, grad, z, params, valid, stats, sums, weights, layer, split_terms):
    frames, features = z.shape
    width = features // 4
    blocks = features // LANES
    whole = lambda array: pl.BlockSpec(array.shape, lambda s, cols, place: (0,) * array.ndim)
    operands = [grad, z, params, valid, stats, sums]
    full = jax.ShapeDtypeStruct((frames, features), F32)
    half = jax.ShapeDtypeStruct((frames, 2 * width), F32)
    terms = [half, half] if split_terms else [full]
    out_shape = [full, half, *terms, jax.ShapeDtypeStruct((3, blocks, LANES), F32)]
    return call(
        partial(norm_back_body, split_terms),
        grid_spec=pltpu.PrefetchScalarGridSpec(
            num_scalar_prefetch=2,
            grid=(2,),
            in_specs=[whole(a) for a in operands] + weight_specs(weights, layer),
            out_specs=[whole(a) for a in out_shape],
            scratch_shapes=[
                pltpu.VMEM((5, blocks, LANES), F32),
                pltpu.VMEM((blocks, LANES), F32),
                pltpu.VMEM((4, frames, width), BF16),
                pltpu.VMEM((4, frames, width), BF16),
            ],
        ),
        out_shape=out_shape,
        cost_estimate=cost(6 * frames * features * features, 4 * features * features),
        name="norm_back",
    )(columns, place, *operands, *weights)


def own_terms_body(n_ups, spots, cols_ref, place_ref, grad_ref, *refs):
    del cols_ref
    ups, refs = refs[:n_ups], refs[n_ups:]
    weights, refs = refs[:4], refs[4:]
    out_ref, high_s, low_s = refs
    width = high_s.shape[2]
    step = pl.program_id(0)

    @pl.when(step == 0)
    def _():
        for block in range(4):
            high, low = split(grad_ref[:, block * width : (block + 1) * width])
            high_s[block] = high
            low_s[block] = low

    value = input_terms(high_s, low_s, weights)
    for pair in range(2):
        at = pl.multiple_of(((place_ref[0] & 1) ^ pair) * width, width)
        out_ref[:, pl.ds(at, width)] = value[:, pair * width : (pair + 1) * width]
    for half in range(2):

        @pl.when(step == half)
        def _():
            first = 2 * half * width
            for (_, column), up in zip(spots, ups):
                low = max(column, first)
                high = min(column + up.shape[1], first + 2 * width)
                if low < high:
                    out_ref[:, low - first : high - first] += up[:, low - column : high - column]


def own_terms(columns, place, grad, ups, weights, layer):
    frames, features = grad.shape
    width = features // 4
    whole = lambda array: pl.BlockSpec(array.shape, lambda s, cols, place: (0,) * array.ndim)
    step_block = pl.BlockSpec((frames, 2 * width), lambda s, cols, place: (0, s))
    return call(
        partial(own_terms_body, len(ups), spots_of_sum(ups, width)),
        grid_spec=pltpu.PrefetchScalarGridSpec(
            num_scalar_prefetch=2,
            grid=(2,),
            in_specs=[whole(grad)]
            + [part_spec(up, frames) for up in ups]
            + weight_specs(weights, layer),
            out_specs=step_block,
            scratch_shapes=[pltpu.VMEM((4, frames, width), BF16)] * 2,
        ),
        out_shape=jax.ShapeDtypeStruct((frames, features), F32),
        cost_estimate=cost(6 * frames * features * features, 4 * features * features),
        name="own_terms",
    )(columns, place, grad, *arrays_of(ups), *weights)


def prepare_body(n_chunks, lists_ref, *refs):
    del lists_ref
    groups = []
    for _ in range(4):
        groups.append(refs[:n_chunks])
        refs = refs[n_chunks:]
    high_ref, low_ref = refs
    padded = high_ref.shape[0] // 2
    for side in range(2):

        @pl.when(pl.program_id(0) // 4 == side)
        def _():
            for clip in range(2):
                row = clip * padded
                for part in groups[2 * clip + side]:
                    rows = part.shape[0]
                    high, low = split(part[...])
                    high_ref[row : row + rows, :] = high
                    low_ref[row : row + rows, :] = low
                    row += rows
                rest = (clip + 1) * padded - row
                zeros = jnp.zeros((rest, high_ref.shape[1]), BF16)
                high_ref[row : row + rest, :] = zeros
                low_ref[row : row + rest, :] = zeros


def prepare(lists, groups):
    width = groups[0][0].shape[1] // 4
    frames = sum(part.shape[0] for part in groups[0])
    padded = -(-frames // LANES) * LANES
    in_specs = []
    for i, group in enumerate(groups):
        for part in group:
            if i % 2 == 0:
                index = lambda s, cols, flip=i // 2: (0, jnp.minimum(s, 3) ^ flip)
            else:
                index = lambda s, cols, flip=i // 2: (0, jnp.maximum(s - 4, 0) ^ flip)
            in_specs.append(pl.BlockSpec((part.shape[0], width), index))
    out = jax.ShapeDtypeStruct((2 * padded, 8 * width), BF16)
    return call(
        partial(prepare_body, len(groups[0])),
        grid_spec=pltpu.PrefetchScalarGridSpec(
            num_scalar_prefetch=1,
            grid=(8,),
            in_specs=in_specs,
            out_specs=[pl.BlockSpec((2 * padded, width), lambda s, cols: (0, cols[s]))] * 2,
        ),
        out_shape=[out, out],
        cost_estimate=cost(0, 16 * frames * 8 * width),
        name="prepare",
    )(lists, *[part for group in groups for part in group])


def product(g_high, g_low, x_high, x_low):
    return dot(g_high, x_high, NN) + (dot(g_high, x_low, NN) + dot(g_low, x_high, NN))


def weight_body(turn, place_ref, *refs):
    if turn:
        grad_ref, near_ref, x_high, x_low, kept, sent, g_high, g_low, t_high, t_low = refs

        @pl.when(pl.program_id(0) == 0)
        def _():
            frames, features = grad_ref.shape
            width = features // 4
            rows = width // 4
            padded = t_high.shape[1] // 2
            t_high[...] = jnp.zeros_like(t_high)
            t_low[...] = jnp.zeros_like(t_low)
            for clip in range(2):
                for dh in range(2):
                    if clip == 0:
                        part = grad_ref[:, 2 * dh * width : (2 * dh + 1) * width]
                    else:
                        part = near_ref[:, dh * width : (dh + 1) * width]
                    high, low = split(part.T)
                    at = (
                        slice(dh * width, (dh + 1) * width),
                        slice(clip * padded, clip * padded + frames),
                    )
                    t_high[at] = high
                    t_low[at] = low
            for group in range(8):
                first, second, dh = group // 4, group // 2 % 2, group % 2
                core = place_ref[6]
                y = place_ref[4] ^ (first * core + second * (1 - core))
                x = place_ref[5] ^ (first * (1 - core) + second * core)
                at = pl.multiple_of(dh * width + (2 * y + x) * rows, rows)
                g_high[group * rows : (group + 1) * rows, :] = t_high[pl.ds(at, rows), :]
                g_low[group * rows : (group + 1) * rows, :] = t_low[pl.ds(at, rows), :]

    else:
        g_high, g_low, x_high, x_low, kept, sent = refs
    half = g_high.shape[0] // 2
    value = product(g_high[...], g_low[...], x_high[...], x_low[...])
    kept[...] = value[:half].reshape(kept.shape)
    sent[...] = value[half:].reshape(sent.shape)


def weight_rows(half, place, grads, x_split, width):
    turn = half == 0
    whole = lambda array: pl.BlockSpec(array.shape, lambda s, place: (0,) * array.ndim)
    x_spec = pl.BlockSpec((x_split[0].shape[0], width), lambda s, place: (0, 4 * half + s))
    shape = (2, 2, width // 4, 4 * width)
    out_shape = [jax.ShapeDtypeStruct(shape, F32)] * 2
    out_specs = [pl.BlockSpec(shape[:3] + (width,), lambda s, place: (0, 0, 0, s))] * 2
    scratch = []
    if turn:
        turned = (2 * width, x_split[0].shape[0])
        out_shape += [jax.ShapeDtypeStruct(turned, BF16)] * 2
        out_specs += [whole(out_shape[-1])] * 2
        scratch = [pltpu.VMEM(turned, BF16)] * 2
    return call(
        partial(weight_body, turn),
        grid_spec=pltpu.PrefetchScalarGridSpec(
            num_scalar_prefetch=1,
            grid=(4,),
            in_specs=[whole(a) for a in grads] + [x_spec] * 2,
            out_specs=out_specs,
            scratch_shapes=scratch,
        ),
        out_shape=out_shape,
        cost_estimate=cost(12 * x_split[0].shape[0] * width * 4 * width, 4 * 8 * width * width),
        name="weight_rows",
    )(place, *grads, *x_split)


def step_body(n, *refs):
    outs = refs[2 * n :]
    column = 0
    for i in range(n):
        total = refs[2 * i][...] + refs[2 * i + 1][...]
        some = slice(column, column + total.shape[-1])
        if len(outs) == 1:
            outs[0][..., some] = total
        else:
            for j, out in enumerate(outs):
                out[..., some] = total[j]
        column += total.shape[-1]


def step_of(*pairs, cut=True):
    shape = list(pairs[0][0].shape)
    shape[-1] = sum(pair[0].shape[-1] for pair in pairs)
    out = jax.ShapeDtypeStruct(tuple(shape[1:] if cut else shape), F32)
    outs = [out, out] if cut else [out]
    whole = lambda array: pl.BlockSpec(array.shape, lambda i: (0,) * array.ndim)
    operands = [array for pair in pairs for array in pair]
    return call(
        partial(step_body, len(pairs)),
        grid=(1,),
        in_specs=[whole(a) for a in operands],
        out_specs=[whole(a) for a in outs],
        out_shape=outs,
        cost_estimate=cost(0, 4 * sum(a.size for a in operands)),
        name="reduction_step",
    )(*operands)


def plane_swap(array, step):
    pairs = []
    for i in range(8):
        over_x = (i % 2 == 0) == (step == 0)
        pairs.append((i, i ^ 2 if over_x else i ^ 4))
    return lax.ppermute(array, ("y", "x", "c"), pairs)


def plane_gather(share, *before):
    first = plane_swap(share, 0)
    second = plane_swap(share, 1)
    return [share, second, first, plane_swap(after(first, *before), 1)]


def assemble_body(groups, place_ref, *refs):
    out_ref = refs[-1]
    core = place_ref[6]
    column = 0
    for group in range(groups):
        rows, columns = refs[4 * group].shape
        for i in range(4):
            first, second = i // 2, i % 2
            y = place_ref[4] ^ (first * core + second * (1 - core))
            x = place_ref[5] ^ (first * (1 - core) + second * core)
            at = pl.multiple_of((2 * y + x) * rows, rows)
            out_ref[..., pl.ds(at, rows), column : column + columns] = refs[4 * group + i][
                ...
            ].reshape(out_ref.shape[:-2] + (rows, columns))
        column += columns


def assemble(place, groups, layer=None, onto=None):
    pieces = [piece for group in groups for piece in group]
    rows = pieces[0].shape[0]
    shape = (4 * rows, sum(group[0].shape[1] for group in groups))
    out_spec = pl.BlockSpec(shape, lambda i: (0, 0))
    aliases, extra, extra_specs = {}, [], []
    if layer is not None:
        out_spec = pl.BlockSpec((1, *shape), lambda i: (layer, 0, 0))
        shape = (LAYERS, *shape)
    if onto is not None:
        aliases, extra = {1 + len(pieces): 0}, [onto]
        extra_specs = [pl.BlockSpec(memory_space=pl.ANY)]
    return call(
        partial(assemble_body, len(groups)),
        grid=(1,),
        out_shape=jax.ShapeDtypeStruct(shape, F32),
        in_specs=[SMEM_SPEC]
        + [pl.BlockSpec(p.shape, lambda i: (0, 0)) for p in pieces]
        + extra_specs,
        out_specs=out_spec,
        input_output_aliases=aliases,
        cost_estimate=cost(0, 8 * shape[-1] * shape[-2]),
        name="assemble",
    )(place, *pieces, *extra)


def half_features(inputs, weights, gains, shifts, decays, biases, lengths, frame_mask, grad_out):
    width, slots = inputs.shape
    clips, frames = frame_mask.shape
    depth = weights.shape[2]
    blocks = 4 * width // LANES
    y, x, h, l, c = (lax.axis_index(name) for name in ("y", "x", "h", "l", "c"))
    b = 2 * y + x
    numbers = [2 * (h ^ (rel // 2)) + (c ^ (rel % 2)) for rel in range(4)] + [y, x, c]
    place = jnp.stack(numbers).astype(jnp.int32)
    own_blocks, other_blocks = (
        jnp.stack(
            [2 * (2 * (h ^ (rel // 2)) + half) + (c ^ (rel % 2)) for rel in range(4)]
        ).astype(jnp.int32)
        for half in (l, 1 - l)
    )
    all_blocks = jnp.concatenate([own_blocks, other_blocks])
    own_columns = jnp.stack([2 * h + l, 2 * (1 - h) + l]).astype(jnp.int32)
    other_columns = jnp.stack([2 * (1 - h) + 1 - l, 2 * h + 1 - l]).astype(jnp.int32)
    rows = width // 4

    clip = 2 * h + c
    seen = lax.dynamic_index_in_dim(frame_mask, clip, 0, keepdims=False)
    length = lax.dynamic_index_in_dim(lengths, clip, 0, keepdims=False)
    moments = jnp.arange(frames, dtype=jnp.int32)
    gate = ((moments < length) & ((seen == 1) | (moments == 0))).astype(F32)
    valid = jnp.broadcast_to(gate[:, None], (frames, LANES))

    def far_share(layer):
        return lax.dynamic_slice(weights, (layer, b * rows, 0), (1, rows, depth))[0]

    def over_h(array):
        return lax.ppermute(array, "h", FLIP2)

    def over_c(array):
        return lax.ppermute(array, "c", FLIP2)

    def over_second(array):
        return plane_swap(array, 1)

    def four_of(near_rows, far_rows):
        return [
            (near_rows, 0),
            (over_c(near_rows), 1),
            (far_rows, 0),
            (over_c(far_rows), 1),
        ]

    near = over_c(weights)
    share = far_share(0)
    close, away = pack(place, after(inputs, share), frames)
    share = over_h(share)
    other_close = swap_half(close)
    up_close, up_away = pack(place, after(grad_out, close), frames)
    params = jnp.stack([gains, shifts + biases, decays], axis=1).reshape(LAYERS, 3, width)
    gathered = lax.all_gather(after(params, up_close), ("h", "c"), axis=2, tiled=True)
    params = gathered.reshape(LAYERS, 3, blocks, LANES)
    share = after(share, gathered, valid)
    away = over_h(after(away, share, other_close))
    far = assemble(place, after([plane_gather(share)], away))
    own = four_of(close, away)
    others = four_of(other_close, swap_half(away))
    half_weights = [[weights, near, far, over_c(far)]]
    share = over_h(after(far_share(1), away))

    saved = []
    chunk_plan = (1, 1)
    for layer in range(LAYERS):
        last = layer == LAYERS - 1
        flat = layer == 0
        if layer > 0:
            others = [(swap_half(array), None) for array, _ in own]
        z, *own_flat = project(
            own_blocks, place, frames, own, half_weights[layer], layer, flat=flat
        )
        if flat:
            share = after(share, z)
            up_away = over_h(after(up_away, share))
        else:
            x_split = prepare(all_blocks, after(groups, z))
            saved[0] = (groups, x_split, *saved[0][2:])
            z = after(z, x_split[0])
        z, stats, *other_flat = project(
            other_blocks, place, frames, others, half_weights[layer], layer, z, valid, flat=flat
        )
        plane = lax.all_gather(stats, ("y", "x"), tiled=True)
        stats = lax.all_gather(plane, ("h", "c"), tiled=True)
        if flat:
            far = assemble(place, after([plane_gather(share, z)], stats))
            half_weights.append([weights, near, far, over_c(far)])
        else:
            upstream = four_of(up_close, after(up_away, plane))
        chunks = chunk_plan[layer]
        state = jnp.zeros((blocks, LANES), F32)
        following, states, slopes = [], [], []
        for chunk in range(chunks):
            *new, kept, slope, state = recur(
                chunk, chunks, place, gate, z, stats, params[layer], valid, state, own, last
            )
            following.extend(new)
            states.append(kept)
            slopes.append(slope)
        if flat:
            groups = [own_flat, other_flat]
        else:
            groups = [arrays_of(own), arrays_of(others)]
        groups += [[over_c(after(p, state)) for p in group] for group in groups]
        saved.append((groups, None, z, stats, states, slopes))
        own = [(array, None) for array in following]
    close, away = following
    away = over_h(away)
    output = four_of(close, away)

    ups = upstream
    results = [None] * LAYERS
    for layer in range(LAYERS - 1, -1, -1):
        groups, x_split, z, stats, states, slopes = saved[layer]
        weight = half_weights[layer]
        grad_pre, sums = back(place, gate, z, stats, params[layer], ups, states, slopes)
        plane = lax.all_gather(sums, ("y", "x"), tiled=True)
        if layer == 0:
            later, go = step_of(*[(k, after(g, plane)) for k, g in zip(stay, come)])
            plane = after(plane, later)
            go = over_second(go)
        sums = lax.all_gather(plane, ("h", "c"), tiled=True)
        grad_z, leaving, *terms, sums = norm_back(
            other_columns, place, grad_pre, z, params[layer], valid, stats, sums, weight, layer,
            layer == 0,
        )
        leaving = over_c(leaving)
        if layer > 0:
            received = [swap_half(terms[0])]
            x_split = prepare(all_blocks, after(groups, grad_z, away))
        else:
            received = [None, swap_half(terms[1])]
            later, go = step_of((later, after(go, grad_z)))
            leaving = after(leaving, later)
            later = (later, over_h(go))
        *first, g_high, g_low = weight_rows(0, place, (grad_z, leaving), x_split, width)
        turned = (g_high, g_low)
        come = [plane_swap(first[1], 0)]
        if layer == 0:
            turned = after(turned, received[1])
            received[0] = swap_half(after(terms[0], received[1]))
        second = weight_rows(1, place, turned, x_split, width)
        come.append(plane_swap(second[1], 0))
        stay = (first[0], second[0])
        kept = own_terms(own_columns, place, after(grad_z, second[0]), ups, weight, layer)
        ups = [(kept, None)] + [(r, None) for r in received]
        results[layer] = lax.dynamic_index_in_dim(
            sums.reshape(3, 4, width), clip, axis=1, keepdims=False
        )

    away = merge(kept, 1, received[1])
    (later,) = step_of((later[0], after(later[1], away)), cut=False)
    away = over_h(away)
    later_first, later_second = plane_swap(later, 0), plane_swap(later, 1)
    total, go = step_of((stay[0], after(come[0], later_first)), (stay[1], come[1]))
    go = over_second(go)
    later = [later, later_second, later_first, plane_swap(after(later_first, total), 1)]
    close = merge(kept, 0, after(received[0], total))
    grad_in = four_of(close, away)
    total, go = step_of((total, after(go, close, grad_in[3][0])))
    go = over_h(go)
    grad_weights = assemble(place, after([later], total), 1)
    output = unpack(place, [(after(array, grad_weights), i) for array, i in output], frames)
    grad_in = unpack(place, [(after(array, output), i) for array, i in grad_in], frames)
    (share,) = step_of((total, after(go, grad_in)), cut=False)
    grad_weights = assemble(place, [plane_gather(share)], 0, grad_weights)
    sums = jnp.stack(results)
    return (
        output,
        grad_in,
        grad_weights,
        sums[:, 0],
        sums[:, 1],
        sums[:, 2],
        sums[:, 1],
    )


def gelu_slope(value):
    return (
        0.5 * (1.0 + jax.scipy.special.erf(value / ROOT_TWO))
        + value * jnp.exp(-0.5 * value * value) / ROOT_TWO_PI
    )


def recur_step(decay, state, inputs):
    drive_t, valid_t = inputs
    pre = drive_t + decay * state
    state = state + valid_t * (jax.nn.gelu(pre, approximate=False) - state)
    return (state, state)


def back_step(decay, carry, inputs):
    upstream_t, valid_t, pre_t = inputs
    total = upstream_t + carry
    grad_pre = total * valid_t * gelu_slope(pre_t)
    carry = total * (1.0 - valid_t) + grad_pre * decay
    return (carry, grad_pre)


def add_piece(weight, piece):
    return jnp.dot(weight, piece, precision=HIGH, preferred_element_type=jnp.float32)


def weight_columns(grad_pre_norm, piece):
    return jnp.einsum("jf,kf->jk", grad_pre_norm, piece, precision=HIGH)


def split_features(inputs, weights, gains, shifts, decays, biases, lengths, frame_mask, grad_out):
    width, slots = inputs.shape
    clips, frames_len = frame_mask.shape
    frames = jnp.arange(frames_len, dtype=jnp.int32)
    valid_grid = (
        (frames[None, :] < lengths[:, None]) & ((frame_mask == 1) | (frames[None, :] == 0))
    ).astype(jnp.float32)
    valid = valid_grid.reshape(-1)
    valid_row = valid[None, :]
    valid_time = jnp.broadcast_to(valid_grid.T[:, :, None], (frames_len, clips, width)).reshape(
        frames_len, clips * width
    )
    count_local = jnp.sum(valid)

    def to_time(array):
        return jnp.transpose(array.reshape(width, clips, frames_len), (2, 1, 0)).reshape(
            frames_len, clips * width
        )

    def from_time(array):
        return jnp.transpose(array.reshape(frames_len, clips, width), (2, 1, 0)).reshape(
            width, slots
        )

    layer_in = inputs
    saved = []
    for layer_no in range(LAYERS):
        weight = weights[layer_no]
        gathered = lax.all_gather(layer_in, "neuron", axis=0, tiled=True)
        pre_norm = add_piece(weight, gathered)
        first_sum, count = lax.psum((jnp.sum(valid_row * pre_norm, axis=1), count_local), "batch")
        mean = first_sum / count
        centered = pre_norm - mean[:, None]
        var = lax.psum(jnp.sum(valid_row * centered * centered, axis=1), "batch") / count
        inv_std = lax.rsqrt(var + EPS)
        zhat = (pre_norm - mean[:, None]) * inv_std[:, None]
        drive = gains[layer_no][:, None] * zhat + (shifts[layer_no] + biases[layer_no])[:, None]
        drive_time = to_time(drive)
        decay_wide = jnp.tile(decays[layer_no], clips)
        start_state = jnp.zeros((clips * width,), jnp.float32)
        _, states = lax.scan(
            partial(recur_step, decay_wide), start_state, (drive_time, valid_time), unroll=8
        )
        saved.append((gathered, zhat, inv_std, drive_time, states, count))
        layer_in = layer_in + valid_row * from_time(states)
    upstream = grad_out
    grad_parts = [None] * LAYERS
    for layer_no in range(LAYERS - 1, -1, -1):
        gathered, zhat, inv_std, drive_time, states, count = saved[layer_no]
        decay_wide = jnp.tile(decays[layer_no], clips)
        gain = gains[layer_no]
        previous = jnp.concatenate([jnp.zeros_like(states[:1]), states[:-1]], axis=0)
        pre_time = drive_time + decay_wide[None, :] * previous
        grad_state = to_time(valid_row * upstream)
        start_carry = jnp.zeros((clips * width,), jnp.float32)
        _, grad_pre_time = lax.scan(
            partial(back_step, decay_wide),
            start_carry,
            (grad_state, valid_time, pre_time),
            reverse=True,
            unroll=8,
        )
        decay_local = jnp.sum(
            jnp.sum(grad_pre_time * previous, axis=0).reshape(clips, width), axis=0
        )
        grad_pre = from_time(grad_pre_time)
        gain_local = jnp.sum(grad_pre * zhat, axis=1)
        shift_local = jnp.sum(grad_pre, axis=1)
        grad_gain, grad_shift, grad_decay = lax.psum(
            (gain_local, shift_local, decay_local), "batch"
        )
        grad_pre_norm = (gain * inv_std)[:, None] * (
            grad_pre - valid_row * (grad_shift[:, None] + zhat * grad_gain[:, None]) / count
        )
        weight_local = weight_columns(grad_pre_norm, gathered)
        input_terms = jnp.einsum("jk,jf->kf", weights[layer_no], grad_pre_norm, precision=HIGH)
        input_grad = lax.psum_scatter(input_terms, "neuron", scatter_dimension=0, tiled=True)
        grad_weight = lax.psum(weight_local, "batch")
        upstream = upstream + input_grad
        grad_parts[layer_no] = (grad_weight, grad_gain, grad_shift, grad_decay)
    grad_weights = jnp.stack([grad_parts[layer_no][0] for layer_no in range(LAYERS)])
    grad_gains = jnp.stack([grad_parts[layer_no][1] for layer_no in range(LAYERS)])
    grad_shifts = jnp.stack([grad_parts[layer_no][2] for layer_no in range(LAYERS)])
    grad_decays = jnp.stack([grad_parts[layer_no][3] for layer_no in range(LAYERS)])
    return (layer_in, upstream, grad_weights, grad_gains, grad_shifts, grad_decays, grad_shifts)


def solution(mesh):
    if (mesh.shape["batch"], mesh.shape["neuron"]) == (4, 8):
        cut = Mesh(mesh.devices.reshape(2, 2, 2, 2, 2), ("y", "x", "h", "l", "c"))
        batch, neuron, body = ("y", "x"), ("h", "l", "c"), half_features
    else:
        cut, batch, neuron, body = mesh, "batch", "neuron", split_features
    in_specs = (
        P(neuron, batch),
        P(None, neuron, None),
        P(None, neuron),
        P(None, neuron),
        P(None, neuron),
        P(None, neuron),
        P(batch),
        P(batch, None),
        P(neuron, batch),
    )
    out_specs = (
        P(neuron, batch),
        P(neuron, batch),
        P(None, neuron, None),
        P(None, neuron),
        P(None, neuron),
        P(None, neuron),
        P(None, neuron),
    )
    return jax.shard_map(
        body, mesh=cut, in_specs=in_specs, out_specs=out_specs, check_vma=False
    )
```

```python
from functools import partial
import math

import jax
import jax.numpy as jnp
from jax import lax
from jax.experimental import pallas as pl
from jax.experimental.pallas import tpu as pltpu
from jax.sharding import Mesh, PartitionSpec as P

LAYERS = 2
EPS = 1e-05
HIGH = lax.Precision.HIGHEST
ROOT_TWO = math.sqrt(2.0)
ROOT_TWO_PI = math.sqrt(2.0 * math.pi)
F32 = jnp.float32
BF16 = jnp.bfloat16
LANES = 128
VMEM_LIMIT = 24 * 1024 * 1024
SMEM_SPEC = pl.BlockSpec(memory_space=pltpu.SMEM)
VMEM_SPEC = pl.BlockSpec(memory_space=pltpu.VMEM)


FLIP2 = [(0, 1), (1, 0)]
DIAGONAL = [(0, 3), (1, 2), (2, 1), (3, 0)]


def swap_half(array):
    return lax.ppermute(array, "l", FLIP2)


def after(value, *others):
    return lax.optimization_barrier((value, others))[0]


def split(value):
    high = value.astype(BF16)
    return high, (value - high.astype(F32)).astype(BF16)


def dot(a, b, dims):
    return lax.dot_general(a, b, (dims, ((), ())), preferred_element_type=F32)


NT = ((1,), (1,))
NN = ((1,), (0,))


def call(body, out_shape, **kwargs):
    in_hbm = lambda a: pltpu.HBM(a.shape, a.dtype)
    return pl.pallas_call(
        body,
        out_shape=jax.tree.map(in_hbm, out_shape),
        compiler_params=pltpu.CompilerParams(vmem_limit_bytes=VMEM_LIMIT),
        **kwargs,
    )


def cost(flops, byte_count):
    return pl.CostEstimate(flops=int(flops) // 64, bytes_accessed=int(byte_count) // 64, transcendentals=0)


def pack_body(frames, place_ref, in_ref, near_ref, far_ref, turned):
    slots = in_ref.shape[1]
    for start in range(0, slots, LANES):
        turned[start : start + LANES, :] = in_ref[:, start : start + LANES].T
    for rel in range(4):
        first = pl.multiple_of(place_ref[rel] * frames, 8)
        out = (near_ref, far_ref)[rel // 2]
        out[(rel % 2) * frames : (rel % 2 + 1) * frames, :] = turned[pl.ds(first, frames), :]


def pack(place, array, frames):
    width, slots = array.shape
    out = jax.ShapeDtypeStruct((2 * frames, width), F32)
    return call(
        partial(pack_body, frames),
        grid=(1,),
        out_shape=[out, out],
        in_specs=[SMEM_SPEC, pl.BlockSpec((width, slots), lambda i: (0, 0))],
        out_specs=[pl.BlockSpec(out.shape, lambda i: (0, 0))] * 2,
        scratch_shapes=[pltpu.VMEM((slots, width), F32)],
        cost_estimate=cost(0, 8 * width * slots),
        name="pack",
    )(place, array)


def part_spec(part, frames):
    array, i = part
    if i is None:
        return pl.BlockSpec(array.shape, lambda *_: (0,) * array.ndim)
    return pl.BlockSpec((frames, array.shape[1]), lambda *_: (i, 0))


def arrays_of(parts):
    return [array for array, _ in parts]


def unpack_body(frames, place_ref, *refs):
    ins, out_ref, turned = refs[:4], refs[4], refs[5]
    slots = out_ref.shape[1]
    for rel in range(4):
        first = pl.multiple_of(place_ref[rel] * frames, 8)
        turned[pl.ds(first, frames), :] = ins[rel][...]
    for start in range(0, slots, LANES):
        out_ref[:, start : start + LANES] = turned[start : start + LANES, :].T


def unpack(place, parts, frames):
    width = parts[0][0].shape[1]
    slots = 4 * frames
    return call(
        partial(unpack_body, frames),
        grid=(1,),
        out_shape=jax.ShapeDtypeStruct((width, slots), F32),
        in_specs=[SMEM_SPEC] + [part_spec(part, frames) for part in parts],
        out_specs=pl.BlockSpec((width, slots), lambda i: (0, 0)),
        scratch_shapes=[pltpu.VMEM((slots, width), F32)],
        cost_estimate=cost(0, 8 * width * slots),
        name="unpack",
    )(place, *arrays_of(parts))


def merge_body(kept_ref, come_ref, out_ref):
    frames, columns = kept_ref.shape
    width = columns // 2
    for i in range(2):
        some = slice(i * width, (i + 1) * width)
        out_ref[i * frames : (i + 1) * frames, :] = kept_ref[:, some] + come_ref[:, some]


def merge(kept, half, come):
    frames, columns = come.shape
    return call(
        merge_body,
        grid=(1,),
        out_shape=jax.ShapeDtypeStruct((2 * frames, columns // 2), F32),
        in_specs=[
            pl.BlockSpec((frames, columns), lambda i: (0, half)),
            pl.BlockSpec((frames, columns), lambda i: (0, 0)),
        ],
        out_specs=pl.BlockSpec((2 * frames, columns // 2), lambda i: (0, 0)),
        cost_estimate=cost(0, 12 * frames * columns),
        name="merge",
    )(kept, come)


def spread_of(parts, width):
    spots, row, column = [], 0, 0
    for array, _ in parts:
        spots.append((row, column))
        if array.shape[1] == width:
            column += width
        else:
            row += array.shape[0]
    return spots


def project_body(n_parts, spots, with_acc, with_stats, with_params, flat, cols_ref, place_ref, *refs):
    del cols_ref
    parts, refs = refs[:n_parts], refs[n_parts:]
    weights, refs = refs[:4], refs[4:]
    if with_acc:
        acc_ref, refs = refs[0], refs[1:]
    if with_stats:
        valid_ref, refs = refs[0], refs[1:]
    if with_params:
        params_ref, refs = refs[0], refs[1:]
    out_ref, refs = refs[0], refs[1:]
    if with_stats:
        stats_ref, refs = refs[0], refs[1:]
    if flat:
        flat_ref, refs = refs[0], refs[1:]
    x_high, x_low = refs
    step = pl.program_id(0)
    width = x_high.shape[2]

    @pl.when(step == 0)
    def _():
        for (row, column), part in zip(spots, parts):
            rows, columns = part.shape
            for start in range(0, columns, width):
                rel = (column + start) // width
                high, low = split(part[:, start : start + width])
                x_high[rel, row : row + rows, :] = high
                x_low[rel, row : row + rows, :] = low
            if flat:
                flat_ref[row : row + rows, column : column + columns] = part[...]
        if with_acc:
            out_ref[...] = acc_ref[...]
        else:
            out_ref[...] = jnp.zeros_like(out_ref)

    stacked = jnp.concatenate([x_high[step], x_low[step], x_high[step]], axis=1)
    for block in range(4):
        w_high, w_low = split(weights[block][...].reshape(width, width))
        columns = slice(block * width, (block + 1) * width)
        out_ref[:, columns] += dot(stacked, jnp.concatenate([w_high, w_high, w_low], axis=1), NT)

    if with_stats:

        @pl.when(step == pl.num_programs(0) - 1)
        def _():
            valid = valid_ref[...]
            own = jnp.sum(valid, axis=0, keepdims=True)
            per = width // LANES
            for row in range(out_ref.shape[1] // LANES):
                z = out_ref[:, row * LANES : (row + 1) * LANES]
                total = jnp.sum(valid * z, axis=0, keepdims=True)
                centred = valid * (z - total / own)
                squares = jnp.sum(centred * centred, axis=0, keepdims=True)
                at = place_ref[row // per] * per + row % per
                stats_ref[0, pl.ds(at, 1), :] = total
                stats_ref[1, pl.ds(at, 1), :] = squares
                stats_ref[2, pl.ds(at, 1), :] = own
            if with_params:
                rest = params_ref.shape[0] - 8
                stats_ref[3] = params_ref[:8, :]
                stats_ref[4] = jnp.zeros_like(stats_ref[4])
                stats_ref[4, :rest, :] = params_ref[8:, :]


def weight_specs(weights, layer, pairs=2):
    specs = []
    for weight in weights:
        width = weight.shape[-2]
        if weight.ndim == 3:
            specs.append(
                pl.BlockSpec((1, width, pairs * width), lambda s, cols, *_: (layer, 0, cols[s]))
            )
        else:
            specs.append(pl.BlockSpec((width, pairs * width), lambda s, cols, *_: (0, cols[s])))
    return specs


def project(
    columns, place, frames, parts, weights, layer, acc=None, valid=None, params=None, flat=False
):
    width = weights[0].shape[-2]
    full = pl.BlockSpec(memory_space=pltpu.VMEM)
    in_specs = [part_spec(part, frames) for part in parts]
    in_specs += weight_specs(weights, layer, 1)
    operands = arrays_of(parts) + list(weights)
    array = jax.ShapeDtypeStruct((frames, 4 * width), F32)
    array_spec = pl.BlockSpec((frames, 4 * width), lambda s, cols, place: (0, 0))
    out_shape, out_specs = [array], [array_spec]
    if acc is not None:
        in_specs.append(full)
        operands.append(acc)
    if valid is not None:
        in_specs.append(full)
        operands.append(valid)
        stats = (3 if params is None else 5, 4 * width // LANES, LANES)
        out_shape.append(jax.ShapeDtypeStruct(stats, F32))
        out_specs.append(pl.BlockSpec(stats, lambda s, cols, place: (0, 0, 0)))
    if params is not None:
        in_specs.append(full)
        operands.append(params)
    if flat:
        out_shape.append(array)
        out_specs.append(array_spec)
    return call(
        partial(
            project_body,
            len(parts),
            spread_of(parts, width),
            acc is not None,
            valid is not None,
            params is not None,
            flat,
        ),
        grid_spec=pltpu.PrefetchScalarGridSpec(
            num_scalar_prefetch=2,
            grid=(4,),
            in_specs=in_specs,
            out_specs=out_specs,
            scratch_shapes=[pltpu.VMEM((4, frames, width), BF16)] * 2,
        ),
        out_shape=out_shape,
        cost_estimate=cost(2 * 3 * frames * 16 * width * width, 4 * 16 * width * width),
        name="project",
    )(columns, place, *operands)


def to_relative(place_ref, spread, rows_ref, value, slot):
    per = value.shape[0] // 4
    spread[...] = value
    for rel in range(4):
        first = place_ref[rel] * per
        for row in range(per):
            rows_ref[slot, rel * per + row : rel * per + row + 1, :] = spread[
                pl.ds(first + row, 1), :
            ]


def tree(values):
    while len(values) > 1:
        values = [a + b for a, b in zip(values[::2], values[1::2])]
    return values[0]


def norm_terms(stats_ref):
    step = stats_ref.shape[0] // 16
    each = [[stats_ref[i] for i in range(slot, stats_ref.shape[0], step)] for slot in range(3)]
    totals, squares, owns = each
    count = tree(owns)
    mean = tree(totals) / count
    away = [total / own - mean for total, own in zip(totals, owns)]
    spread = tree([s + n * a * a for s, n, a in zip(squares, owns, away)])
    return count, mean, lax.rsqrt(spread / count + EPS)


def recur_body(n_parts, spots, last, layer, spread_params, place_ref, gate_ref, z_ref, stats_ref, params_ref, valid_ref, *refs):
    parts, refs = refs[:n_parts], refs[n_parts:]
    outs, refs = refs[: 1 + last], refs[1 + last :]
    if spread_params:
        state_ref, slope_ref, params_out, rows, spread, drive_s, state_s, slope_s = refs
    else:
        state_ref, slope_ref, rows, spread, drive_s, state_s, slope_s = refs
    frames = z_ref.shape[0]
    blocks = z_ref.shape[1] // LANES
    per = blocks // 4
    if spread_params:
        for rel in range(4):
            first = place_ref[rel] * (stats_ref.shape[0] // 16)
            for row in range(LAYERS * 3 * per):
                params_out[row // per, rel * per + row % per : rel * per + row % per + 1, :] = (
                    stats_ref[first + 3 + row // 8, row % 8 : row % 8 + 1, :]
                )
        params = [params_out[3 * layer + i] for i in range(3)]
    else:
        params = [params_ref[3 * layer + i] for i in range(3)]
    _, mean, inv_std = norm_terms(stats_ref)
    to_relative(place_ref, spread, rows, mean, 0)
    to_relative(place_ref, spread, rows, inv_std, 1)
    rows[1] = rows[1] * params[0]
    rows[2] = params[1]
    decay = params[2]
    for row in range(blocks):
        z = z_ref[:, row * LANES : (row + 1) * LANES]
        drive_s[row * frames : (row + 1) * frames, :] = (
            z - rows[0, row : row + 1, :]
        ) * rows[1, row : row + 1, :] + rows[2, row : row + 1, :]

    def step(t, state):
        at = pl.ds(t, blocks, stride=frames)
        pre = drive_s[at, :] + decay * state
        half = 0.5 + 0.5 * lax.erf(pre * (1.0 / ROOT_TWO))
        gate = gate_ref[t] > 0.0
        slope = half + pre * jnp.exp(-0.5 * pre * pre) * (1.0 / ROOT_TWO_PI)
        state = jnp.where(gate, pre * half, state)
        state_s[at, :] = state
        slope_s[at, :] = jnp.where(gate, slope, 0.0)
        return state

    lax.fori_loop(0, frames, step, jnp.zeros((blocks, LANES), F32), unroll=8)
    valid = valid_ref[...]
    for row in range(blocks):
        lanes = slice(row * LANES, (row + 1) * LANES)
        state = state_s[row * frames : (row + 1) * frames, :]
        state_ref[:, lanes] = state
        slope_ref[:, lanes] = slope_s[row * frames : (row + 1) * frames, :]
        for (top, column), part in zip(spots, parts):
            if column <= row * LANES < column + part.shape[1]:
                x = part[:, row * LANES - column : (row + 1) * LANES - column]
                some = slice(top, top + part.shape[0])
                value = x + valid[some] * state[some]
                if last:
                    rel, at = divmod(row * LANES, outs[0].shape[1])
                    base = (rel % 2) * frames + top
                    outs[rel // 2][base : base + part.shape[0], at : at + LANES] = value
                else:
                    outs[0][top : top + part.shape[0], lanes] = value


def recur(layer, place, gate, z, stats, params, valid, parts, last):
    frames, features = z.shape
    width = features // 4
    blocks = features // LANES
    whole = lambda array: pl.BlockSpec(array.shape, lambda i: (0,) * array.ndim)
    full = jax.ShapeDtypeStruct((frames, features), F32)
    outs = [jax.ShapeDtypeStruct((2 * frames, width), F32)] * 2 if last else [full]
    out_shape = outs + [full, full]
    spread_params = params is None
    if spread_params:
        out_shape.append(jax.ShapeDtypeStruct((3 * LAYERS, blocks, LANES), F32))
        params = valid
    return call(
        partial(recur_body, len(parts), spread_of(parts, width), last, layer, spread_params),
        grid=(1,),
        in_specs=[SMEM_SPEC, SMEM_SPEC]
        + [whole(a) for a in (z, stats, params, valid)]
        + [part_spec(part, frames) for part in parts],
        out_specs=[whole(s) for s in out_shape],
        out_shape=out_shape,
        scratch_shapes=[
            pltpu.VMEM((3, blocks, LANES), F32),
            pltpu.VMEM((blocks, LANES), F32),
        ]
        + [pltpu.VMEM((blocks * frames, LANES), F32)] * 3,
        cost_estimate=cost(100 * frames * features, 20 * frames * features),
        name="recur",
    )(place, gate, z, stats, params, valid, *arrays_of(parts))


def back_body(n_parts, spots, n_state, layer, place_ref, gate_ref, z_ref, stats_ref, params_ref, *refs):
    parts, refs = refs[:n_parts], refs[n_parts:]
    states, refs = refs[:n_state], refs[n_state:]
    slopes, refs = refs[:n_state], refs[n_state:]
    grad_ref, sums_ref, rows, spread, up_s, state_s, slope_s = refs
    frames = z_ref.shape[0]
    blocks = z_ref.shape[1] // LANES
    tall = frames + 8
    _, mean, inv_std = norm_terms(stats_ref)
    to_relative(place_ref, spread, rows, mean, 0)
    to_relative(place_ref, spread, rows, inv_std, 1)
    for row in range(blocks):
        lanes = slice(row * LANES, (row + 1) * LANES)
        base = row * frames
        up = None
        for (top, column), part in zip(spots, parts):
            if column <= row * LANES < column + part.shape[1] and part.shape[0] == frames:
                value = part[:, row * LANES - column : (row + 1) * LANES - column]
                up = value if up is None else up + value
        up_s[base : base + frames, :] = up
        state_s[row * tall : row * tall + 8, :] = jnp.zeros((8, LANES), F32)
        first = 0
        for state, slope in zip(states, slopes):
            some = state.shape[0]
            at = row * tall + 8 + first
            state_s[at : at + some, :] = state[:, lanes]
            slope_s[base + first : base + first + some, :] = slope[:, lanes]
            first += some
    decay = params_ref[3 * layer + 2]

    def step(i, carry):
        t = frames - 1 - i
        at = pl.ds(t, blocks, stride=frames)
        slope = slope_s[at, :]
        gate = gate_ref[t]
        total = gate * up_s[at, :] + carry
        up_s[at, :] = total * slope
        return total * (slope * decay + (1.0 - gate))

    lax.fori_loop(0, frames, step, jnp.zeros((blocks, LANES), F32), unroll=8)
    per = blocks // 4
    for row in range(blocks):
        lanes = slice(row * LANES, (row + 1) * LANES)
        base = row * frames
        grad = up_s[base : base + frames, :]
        grad_ref[:, lanes] = grad
        zhat = (z_ref[:, lanes] - rows[0, row : row + 1, :]) * rows[1, row : row + 1, :]
        before = state_s[row * tall + 7 : row * tall + 7 + frames, :]
        at = place_ref[row // per] * per + row % per
        for slot, value in enumerate((grad * zhat, grad, grad * before)):
            sums_ref[slot, pl.ds(at, 1), :] = jnp.sum(value, axis=0, keepdims=True)


def spots_of_sum(parts, width):
    spots, column = [], 0
    for array, _ in parts:
        spots.append((0, column % (4 * width)))
        column += array.shape[1]
    return spots


def back(layer, place, gate, z, stats, params, ups, states, slopes):
    frames, features = z.shape
    width = features // 4
    blocks = features // LANES
    whole = lambda array: pl.BlockSpec(array.shape, lambda i: (0,) * array.ndim)
    out_shape = [
        jax.ShapeDtypeStruct((frames, features), F32),
        jax.ShapeDtypeStruct((3, blocks, LANES), F32),
    ]
    return call(
        partial(back_body, len(ups), spots_of_sum(ups, width), len(states), layer),
        grid=(1,),
        in_specs=[SMEM_SPEC] * 2
        + [whole(a) for a in (z, stats, params)]
        + [part_spec(up, frames) for up in ups]
        + [whole(a) for a in (*states, *slopes)],
        out_specs=[whole(a) for a in out_shape],
        out_shape=out_shape,
        scratch_shapes=[
            pltpu.VMEM((2, blocks, LANES), F32),
            pltpu.VMEM((blocks, LANES), F32),
            pltpu.VMEM((blocks * frames, LANES), F32),
            pltpu.VMEM((blocks * (frames + 8), LANES), F32),
            pltpu.VMEM((blocks * frames, LANES), F32),
        ],
        cost_estimate=cost(30 * frames * features, 20 * frames * features),
        name="back",
    )(place, gate, z, stats, params, *arrays_of(ups), *states, *slopes)


def input_terms(high_s, low_s, weights):
    width = high_s.shape[2]
    left, right = [], []
    for block, weight in enumerate(weights):
        w_high, w_low = split(weight[...].reshape(width, 2 * width))
        left += [high_s[block], low_s[block], high_s[block]]
        right += [w_high, w_high, w_low]
    return dot(jnp.concatenate(left, axis=1), jnp.concatenate(right, axis=0), NN)


def norm_back_body(split_terms, layer, cols_ref, place_ref, grad_ref, z_ref, params_ref, valid_ref, stats_ref, sums_ref, *refs):
    del cols_ref
    weights, refs = refs[:4], refs[4:]
    if split_terms:
        out_ref, leave_ref, near_term_ref, far_term_ref, sums_out_ref, *refs = refs
        term_refs, starts = (far_term_ref, near_term_ref), (0, 0)
    else:
        out_ref, leave_ref, term_ref, sums_out_ref, *refs = refs
        term_refs, starts = (term_ref, term_ref), (2 * grad_ref.shape[1] // 4, 0)
    rows, spread, high_s, low_s = refs
    blocks = z_ref.shape[1] // LANES
    width = high_s.shape[2]
    per = width // LANES

    @pl.when(pl.program_id(0) == 0)
    def _():
        count, mean, inv_std = norm_terms(stats_ref)
        to_relative(place_ref, spread, rows, mean, 0)
        to_relative(place_ref, spread, rows, inv_std, 1)
        rows[2] = rows[1] * params_ref[3 * layer]
        sums = tree([sums_ref[i : i + 3] for i in range(0, sums_ref.shape[0], 3)])
        sums_out_ref[...] = sums
        to_relative(place_ref, spread, rows, sums[0] / count, 3)
        to_relative(place_ref, spread, rows, sums[1] / count, 4)
        valid = valid_ref[...]
        for row in range(blocks):
            lanes = slice(row * LANES, (row + 1) * LANES)
            one = lambda slot: rows[slot, row : row + 1, :]
            zhat = (z_ref[:, lanes] - one(0)) * one(1)
            value = one(2) * (grad_ref[:, lanes] - valid * (one(4) + zhat * one(3)))
            out_ref[:, lanes] = value
            if (row // per) % 2:
                at = (row // per // 2) * width + (row % per) * LANES
                leave_ref[:, at : at + LANES] = value
            high, low = split(value)
            inner = slice((row % per) * LANES, (row % per + 1) * LANES)
            high_s[row // per, :, inner] = high
            low_s[row // per, :, inner] = low

    value = input_terms(high_s, low_s, weights)
    for step, (term_ref, first) in enumerate(zip(term_refs, starts)):

        @pl.when(pl.program_id(0) == step)
        def _():
            for pair in range(2):
                at = pl.multiple_of(((place_ref[0] & 1) ^ pair) * width, width)
                term_ref[:, pl.ds(first + at, width)] = value[
                    :, pair * width : (pair + 1) * width
                ]


def norm_back(columns, place, grad, z, params, valid, stats, sums, weights, layer, split_terms):
    frames, features = z.shape
    width = features // 4
    blocks = features // LANES
    whole = lambda array: pl.BlockSpec(array.shape, lambda s, cols, place: (0,) * array.ndim)
    operands = [grad, z, params, valid, stats, sums]
    full = jax.ShapeDtypeStruct((frames, features), F32)
    half = jax.ShapeDtypeStruct((frames, 2 * width), F32)
    terms = [half, half] if split_terms else [full]
    out_shape = [full, half, *terms, jax.ShapeDtypeStruct((3, blocks, LANES), F32)]
    return call(
        partial(norm_back_body, split_terms, layer),
        grid_spec=pltpu.PrefetchScalarGridSpec(
            num_scalar_prefetch=2,
            grid=(2,),
            in_specs=[whole(a) for a in operands] + weight_specs(weights, layer),
            out_specs=[whole(a) for a in out_shape],
            scratch_shapes=[
                pltpu.VMEM((5, blocks, LANES), F32),
                pltpu.VMEM((blocks, LANES), F32),
                pltpu.VMEM((4, frames, width), BF16),
                pltpu.VMEM((4, frames, width), BF16),
            ],
        ),
        out_shape=out_shape,
        cost_estimate=cost(6 * frames * features * features, 4 * features * features),
        name="norm_back",
    )(columns, place, *operands, *weights)


def own_terms_body(n_ups, spots, cols_ref, place_ref, grad_ref, *refs):
    del cols_ref
    ups, refs = refs[:n_ups], refs[n_ups:]
    weights, refs = refs[:4], refs[4:]
    out_ref, high_s, low_s = refs
    width = high_s.shape[2]
    step = pl.program_id(0)

    @pl.when(step == 0)
    def _():
        for block in range(4):
            high, low = split(grad_ref[:, block * width : (block + 1) * width])
            high_s[block] = high
            low_s[block] = low

    value = input_terms(high_s, low_s, weights)
    for pair in range(2):
        at = pl.multiple_of(((place_ref[0] & 1) ^ pair) * width, width)
        out_ref[:, pl.ds(at, width)] = value[:, pair * width : (pair + 1) * width]
    for half in range(2):

        @pl.when(step == half)
        def _():
            first = 2 * half * width
            for (_, column), up in zip(spots, ups):
                low = max(column, first)
                high = min(column + up.shape[1], first + 2 * width)
                if low < high:
                    out_ref[:, low - first : high - first] += up[:, low - column : high - column]


def own_terms(columns, place, grad, ups, weights, layer):
    frames, features = grad.shape
    width = features // 4
    whole = lambda array: pl.BlockSpec(array.shape, lambda s, cols, place: (0,) * array.ndim)
    step_block = pl.BlockSpec((frames, 2 * width), lambda s, cols, place: (0, s))
    return call(
        partial(own_terms_body, len(ups), spots_of_sum(ups, width)),
        grid_spec=pltpu.PrefetchScalarGridSpec(
            num_scalar_prefetch=2,
            grid=(2,),
            in_specs=[whole(grad)]
            + [part_spec(up, frames) for up in ups]
            + weight_specs(weights, layer),
            out_specs=step_block,
            scratch_shapes=[pltpu.VMEM((4, frames, width), BF16)] * 2,
        ),
        out_shape=jax.ShapeDtypeStruct((frames, features), F32),
        cost_estimate=cost(6 * frames * features * features, 4 * features * features),
        name="own_terms",
    )(columns, place, grad, *arrays_of(ups), *weights)


def prepare_body(n_chunks, lists_ref, *refs):
    del lists_ref
    groups = []
    for _ in range(4):
        groups.append(refs[:n_chunks])
        refs = refs[n_chunks:]
    high_ref, low_ref = refs
    padded = high_ref.shape[0] // 2
    for side in range(2):

        @pl.when(pl.program_id(0) // 4 == side)
        def _():
            for clip in range(2):
                row = clip * padded
                for part in groups[2 * clip + side]:
                    rows = part.shape[0]
                    high, low = split(part[...])
                    high_ref[row : row + rows, :] = high
                    low_ref[row : row + rows, :] = low
                    row += rows
                rest = (clip + 1) * padded - row
                zeros = jnp.zeros((rest, high_ref.shape[1]), BF16)
                high_ref[row : row + rest, :] = zeros
                low_ref[row : row + rest, :] = zeros


def prepare(lists, groups):
    width = groups[0][0].shape[1] // 4
    frames = sum(part.shape[0] for part in groups[0])
    padded = -(-frames // LANES) * LANES
    in_specs = []
    for i, group in enumerate(groups):
        for part in group:
            if i % 2 == 0:
                index = lambda s, cols, flip=i // 2: (0, jnp.minimum(s, 3) ^ flip)
            else:
                index = lambda s, cols, flip=i // 2: (0, jnp.maximum(s - 4, 0) ^ flip)
            in_specs.append(pl.BlockSpec((part.shape[0], width), index))
    out = jax.ShapeDtypeStruct((2 * padded, 8 * width), BF16)
    return call(
        partial(prepare_body, len(groups[0])),
        grid_spec=pltpu.PrefetchScalarGridSpec(
            num_scalar_prefetch=1,
            grid=(8,),
            in_specs=in_specs,
            out_specs=[pl.BlockSpec((2 * padded, width), lambda s, cols: (0, cols[s]))] * 2,
        ),
        out_shape=[out, out],
        cost_estimate=cost(0, 16 * frames * 8 * width),
        name="prepare",
    )(lists, *[part for group in groups for part in group])


def product(g_high, g_low, x_high, x_low):
    return dot(g_high, x_high, NN) + (dot(g_high, x_low, NN) + dot(g_low, x_high, NN))


def weight_body(turn, place_ref, *refs):
    if turn:
        grad_ref, near_ref, x_high, x_low, kept, sent, g_high, g_low, t_high, t_low = refs

        @pl.when(pl.program_id(0) == 0)
        def _():
            frames, features = grad_ref.shape
            width = features // 4
            rows = width // 4
            padded = t_high.shape[1] // 2
            t_high[...] = jnp.zeros_like(t_high)
            t_low[...] = jnp.zeros_like(t_low)
            for clip in range(2):
                for dh in range(2):
                    if clip == 0:
                        part = grad_ref[:, 2 * dh * width : (2 * dh + 1) * width]
                    else:
                        part = near_ref[:, dh * width : (dh + 1) * width]
                    high, low = split(part.T)
                    at = (
                        slice(dh * width, (dh + 1) * width),
                        slice(clip * padded, clip * padded + frames),
                    )
                    t_high[at] = high
                    t_low[at] = low
            for group in range(8):
                first, second, dh = group // 4, group // 2 % 2, group % 2
                core = place_ref[6]
                y = place_ref[4] ^ (first * core + second * (1 - core))
                x = place_ref[5] ^ (first * (1 - core) + second * core)
                at = pl.multiple_of(dh * width + (2 * y + x) * rows, rows)
                g_high[group * rows : (group + 1) * rows, :] = t_high[pl.ds(at, rows), :]
                g_low[group * rows : (group + 1) * rows, :] = t_low[pl.ds(at, rows), :]

    else:
        g_high, g_low, x_high, x_low, kept, sent = refs
    half = g_high.shape[0] // 2
    value = product(g_high[...], g_low[...], x_high[...], x_low[...])
    kept[...] = value[:half].reshape(kept.shape)
    sent[...] = value[half:].reshape(sent.shape)


def weight_rows(half, place, grads, x_split, width):
    turn = half == 0
    whole = lambda array: pl.BlockSpec(array.shape, lambda s, place: (0,) * array.ndim)
    x_spec = pl.BlockSpec((x_split[0].shape[0], width), lambda s, place: (0, 4 * half + s))
    shape = (2, 2, width // 4, 4 * width)
    out_shape = [jax.ShapeDtypeStruct(shape, F32)] * 2
    out_specs = [pl.BlockSpec(shape[:3] + (width,), lambda s, place: (0, 0, 0, s))] * 2
    scratch = []
    if turn:
        turned = (2 * width, x_split[0].shape[0])
        out_shape += [jax.ShapeDtypeStruct(turned, BF16)] * 2
        out_specs += [whole(out_shape[-1])] * 2
        scratch = [pltpu.VMEM(turned, BF16)] * 2
    return call(
        partial(weight_body, turn),
        grid_spec=pltpu.PrefetchScalarGridSpec(
            num_scalar_prefetch=1,
            grid=(4,),
            in_specs=[whole(a) for a in grads] + [x_spec] * 2,
            out_specs=out_specs,
            scratch_shapes=scratch,
        ),
        out_shape=out_shape,
        cost_estimate=cost(12 * x_split[0].shape[0] * width * 4 * width, 4 * 8 * width * width),
        name="weight_rows",
    )(place, *grads, *x_split)


def step_body(n, *refs):
    outs = refs[2 * n :]
    column = 0
    for i in range(n):
        total = refs[2 * i][...] + refs[2 * i + 1][...]
        some = slice(column, column + total.shape[-1])
        if len(outs) == 1:
            outs[0][..., some] = total
        else:
            for j, out in enumerate(outs):
                out[..., some] = total[j]
        column += total.shape[-1]


def step_of(*pairs, cut=True):
    shape = list(pairs[0][0].shape)
    shape[-1] = sum(pair[0].shape[-1] for pair in pairs)
    out = jax.ShapeDtypeStruct(tuple(shape[1:] if cut else shape), F32)
    outs = [out, out] if cut else [out]
    whole = lambda array: pl.BlockSpec(array.shape, lambda i: (0,) * array.ndim)
    operands = [array for pair in pairs for array in pair]
    return call(
        partial(step_body, len(pairs)),
        grid=(1,),
        in_specs=[whole(a) for a in operands],
        out_specs=[whole(a) for a in outs],
        out_shape=outs,
        cost_estimate=cost(0, 4 * sum(a.size for a in operands)),
        name="reduction_step",
    )(*operands)


def plane_swap(array, step):
    pairs = []
    for i in range(8):
        over_x = (i % 2 == 0) == (step == 0)
        pairs.append((i, i ^ 2 if over_x else i ^ 4))
    return lax.ppermute(array, ("y", "x", "c"), pairs)


def plane_gather(share, *before):
    first = plane_swap(share, 0)
    second = plane_swap(share, 1)
    return [share, second, first, plane_swap(after(first, *before), 1)]


def assemble_body(groups, by_core, place_ref, *refs):
    out_ref = refs[-1]
    core = place_ref[6] if by_core else 0
    column = 0
    for group in range(groups):
        rows, columns = refs[4 * group].shape
        for i in range(4):
            first, second = i // 2, i % 2
            if by_core:
                first, second = (
                    first * core + second * (1 - core),
                    first * (1 - core) + second * core,
                )
            at = pl.multiple_of((2 * (place_ref[4] ^ first) + (place_ref[5] ^ second)) * rows, rows)
            out_ref[..., pl.ds(at, rows), column : column + columns] = refs[4 * group + i][
                ...
            ].reshape(out_ref.shape[:-2] + (rows, columns))
        column += columns


def assemble(place, groups, layer=None, onto=None, by_core=True):
    pieces = [piece for group in groups for piece in group]
    rows = pieces[0].shape[0]
    shape = (4 * rows, sum(group[0].shape[1] for group in groups))
    out_spec = pl.BlockSpec(shape, lambda i: (0, 0))
    aliases, extra, extra_specs = {}, [], []
    if layer is not None:
        out_spec = pl.BlockSpec((1, *shape), lambda i: (layer, 0, 0))
        shape = (LAYERS, *shape)
    if onto is not None:
        aliases, extra = {1 + len(pieces): 0}, [onto]
        extra_specs = [pl.BlockSpec(memory_space=pl.ANY)]
    return call(
        partial(assemble_body, len(groups), by_core),
        grid=(1,),
        out_shape=jax.ShapeDtypeStruct(shape, F32),
        in_specs=[SMEM_SPEC]
        + [pl.BlockSpec(p.shape, lambda i: (0, 0)) for p in pieces]
        + extra_specs,
        out_specs=out_spec,
        input_output_aliases=aliases,
        cost_estimate=cost(0, 8 * shape[-1] * shape[-2]),
        name="assemble",
    )(place, *pieces, *extra)


def half_features(inputs, weights, gains, shifts, decays, biases, lengths, frame_mask, grad_out):
    width, slots = inputs.shape
    clips, frames = frame_mask.shape
    depth = weights.shape[2]
    blocks = 4 * width // LANES
    y, x, h, l, c = (lax.axis_index(name) for name in ("y", "x", "h", "l", "c"))
    b = 2 * y + x
    numbers = [2 * (h ^ (rel // 2)) + (c ^ (rel % 2)) for rel in range(4)] + [y, x, c]
    place = jnp.stack(numbers).astype(jnp.int32)
    own_blocks, other_blocks = (
        jnp.stack(
            [2 * (2 * (h ^ (rel // 2)) + half) + (c ^ (rel % 2)) for rel in range(4)]
        ).astype(jnp.int32)
        for half in (l, 1 - l)
    )
    all_blocks = jnp.concatenate([own_blocks, other_blocks])
    own_columns = jnp.stack([2 * h + l, 2 * (1 - h) + l]).astype(jnp.int32)
    other_columns = jnp.stack([2 * (1 - h) + 1 - l, 2 * h + 1 - l]).astype(jnp.int32)
    rows = width // 4

    clip = 2 * h + c
    seen = lax.dynamic_index_in_dim(frame_mask, clip, 0, keepdims=False)
    length = lax.dynamic_index_in_dim(lengths, clip, 0, keepdims=False)
    moments = jnp.arange(frames, dtype=jnp.int32)
    gate = ((moments < length) & ((seen == 1) | (moments == 0))).astype(F32)
    valid = jnp.broadcast_to(gate[:, None], (frames, LANES))

    def far_share(layer):
        return lax.dynamic_slice(weights, (layer, b * rows, 0), (1, rows, depth))[0]

    def over_h(array):
        return lax.ppermute(array, "h", FLIP2)

    def over_c(array):
        return lax.ppermute(array, "c", FLIP2)

    def over_second(array):
        return plane_swap(array, 1)

    def four_of(near_rows, far_rows):
        return [
            (near_rows, 0),
            (over_c(near_rows), 1),
            (far_rows, 0),
            (over_c(far_rows), 1),
        ]

    def far_blocks(share):
        both = lax.ppermute(share, ("y", "x"), DIAGONAL)
        shares = [share, lax.ppermute(share, "x", FLIP2), lax.ppermute(share, "y", FLIP2), both]
        other = [over_c(piece) for piece in shares]
        return [assemble(place, [pieces], by_core=False) for pieces in (shares, other)]

    near = over_c(weights)
    share = far_share(0)
    close, away = pack(place, after(inputs, share), frames)
    share = over_h(share)
    away = over_h(away)
    other_close = swap_half(close)
    up_close, up_away = pack(place, after(grad_out, close), frames)
    share = after(share, up_close, valid)
    own = four_of(close, away)
    other_away = swap_half(away)
    half_weights = [[weights, near, *far_blocks(share)]]
    params = jnp.stack([gains, shifts + biases, decays], axis=1)
    own_params = params.reshape(LAYERS * 3 * width // LANES, LANES)
    params = None

    saved = []
    for layer in range(LAYERS):
        last = layer == LAYERS - 1
        flat = layer == 0
        if layer > 0:
            others = [(swap_half(array), None) for array, _ in own]
        z, *own_flat = project(
            own_blocks, place, frames, own, half_weights[layer], layer, flat=flat
        )
        if flat:
            others = four_of(other_close, after(other_away, z))
        z, stats, *other_flat = project(
            other_blocks,
            place,
            frames,
            others,
            half_weights[layer],
            layer,
            z,
            valid,
            own_params if flat else None,
            flat,
        )
        if last:
            upstream = four_of(up_close, after(up_away, z))
        if flat:
            stats = lax.all_gather(stats, ("h", "c"), tiled=True)
            share = over_h(after(far_share(1), stats))
            stats = lax.all_gather(stats, ("y", "x"), tiled=True)
        else:
            stats = lax.all_gather(stats, ("y", "x"), tiled=True)
            stats = lax.all_gather(stats, ("h", "c"), tiled=True)
        *following, states, slopes = recur(
            layer, place, gate, z, stats, params, valid, own, last
        )
        if flat:
            *following, states, slopes, params = *following, states, slopes
            groups = [own_flat, other_flat]
        else:
            groups = [arrays_of(own), arrays_of(others)]
        groups += [[over_c(after(p, z)) for p in group] for group in groups]
        x_split = prepare(all_blocks, after(groups, slopes)) if flat else None
        if flat:
            up_away = over_h(after(up_away, x_split[0], share))
            half_weights.append([weights, near, *far_blocks(after(share, slopes))])
        saved.append((groups, x_split, z, stats, states, slopes))
        own = [(array, None) for array in following]
    close, away = following
    away = over_h(away)
    output = four_of(close, away)

    ups = upstream
    results = [None] * LAYERS
    for layer in range(LAYERS - 1, -1, -1):
        groups, x_split, z, stats, states, slopes = saved[layer]
        weight = half_weights[layer]
        grad_pre, sums = back(
            layer, place, gate, z, stats, params, ups, [states], [slopes]
        )
        plane = lax.all_gather(sums, ("y", "x"), tiled=True)
        if layer == 0:
            later, go = step_of(*[(k, after(g, plane)) for k, g in zip(stay, come)])
            plane = after(plane, later)
            go = over_second(go)
        sums = lax.all_gather(plane, ("h", "c"), tiled=True)
        grad_z, leaving, *terms, sums = norm_back(
            other_columns, place, grad_pre, z, params, valid, stats, sums, weight, layer,
            layer == 0,
        )
        leaving = over_c(leaving)
        if layer > 0:
            received = [swap_half(terms[0])]
            x_split = prepare(all_blocks, after(groups, grad_z, away))
        else:
            received = [None, swap_half(terms[1])]
            later, go = step_of((later, after(go, grad_z)))
            leaving = after(leaving, later)
            later = (later, over_h(go))
        *first, g_high, g_low = weight_rows(0, place, (grad_z, leaving), x_split, width)
        turned = (g_high, g_low)
        come = [plane_swap(first[1], 0)]
        if layer == 0:
            received[0] = swap_half(after(terms[0], received[1]))
        second = weight_rows(1, place, turned, x_split, width)
        come.append(plane_swap(second[1], 0))
        stay = (first[0], second[0])
        kept = own_terms(own_columns, place, after(grad_z, second[0]), ups, weight, layer)
        ups = [(kept, None)] + [(r, None) for r in received]
        results[layer] = lax.dynamic_index_in_dim(
            sums.reshape(3, 4, width), clip, axis=1, keepdims=False
        )

    away = merge(kept, 1, received[1])
    (later,) = step_of((later[0], after(later[1], away)), cut=False)
    away = over_h(away)
    later_first, later_second = plane_swap(later, 0), plane_swap(later, 1)
    total, go = step_of((stay[0], after(come[0], later_first)), (stay[1], come[1]))
    go = over_second(go)
    later = [later, later_second, later_first, plane_swap(after(later_first, total), 1)]
    close = merge(kept, 0, after(received[0], total))
    grad_in = four_of(close, away)
    total, go = step_of((total, after(go, close, grad_in[3][0])))
    go = over_h(go)
    grad_weights = assemble(place, after([later], total), 1)
    output = unpack(place, [(after(array, grad_weights), i) for array, i in output], frames)
    grad_in = unpack(place, [(after(array, output), i) for array, i in grad_in], frames)
    (share,) = step_of((total, after(go, grad_in)), cut=False)
    grad_weights = assemble(place, [plane_gather(share)], 0, grad_weights)
    sums = jnp.stack(results)
    return (
        output,
        grad_in,
        grad_weights,
        sums[:, 0],
        sums[:, 1],
        sums[:, 2],
        sums[:, 1],
    )


def gelu_slope(value):
    return (
        0.5 * (1.0 + jax.scipy.special.erf(value / ROOT_TWO))
        + value * jnp.exp(-0.5 * value * value) / ROOT_TWO_PI
    )


def recur_step(decay, state, inputs):
    drive_t, valid_t = inputs
    pre = drive_t + decay * state
    state = state + valid_t * (jax.nn.gelu(pre, approximate=False) - state)
    return (state, state)


def back_step(decay, carry, inputs):
    upstream_t, valid_t, pre_t = inputs
    total = upstream_t + carry
    grad_pre = total * valid_t * gelu_slope(pre_t)
    carry = total * (1.0 - valid_t) + grad_pre * decay
    return (carry, grad_pre)


def add_piece(weight, piece):
    return jnp.dot(weight, piece, precision=HIGH, preferred_element_type=jnp.float32)


def weight_columns(grad_pre_norm, piece):
    return jnp.einsum("jf,kf->jk", grad_pre_norm, piece, precision=HIGH)


def split_features(inputs, weights, gains, shifts, decays, biases, lengths, frame_mask, grad_out):
    width, slots = inputs.shape
    clips, frames_len = frame_mask.shape
    frames = jnp.arange(frames_len, dtype=jnp.int32)
    valid_grid = (
        (frames[None, :] < lengths[:, None]) & ((frame_mask == 1) | (frames[None, :] == 0))
    ).astype(jnp.float32)
    valid = valid_grid.reshape(-1)
    valid_row = valid[None, :]
    valid_time = jnp.broadcast_to(valid_grid.T[:, :, None], (frames_len, clips, width)).reshape(
        frames_len, clips * width
    )
    count_local = jnp.sum(valid)

    def to_time(array):
        return jnp.transpose(array.reshape(width, clips, frames_len), (2, 1, 0)).reshape(
            frames_len, clips * width
        )

    def from_time(array):
        return jnp.transpose(array.reshape(frames_len, clips, width), (2, 1, 0)).reshape(
            width, slots
        )

    layer_in = inputs
    saved = []
    for layer_no in range(LAYERS):
        weight = weights[layer_no]
        gathered = lax.all_gather(layer_in, "neuron", axis=0, tiled=True)
        pre_norm = add_piece(weight, gathered)
        first_sum, count = lax.psum((jnp.sum(valid_row * pre_norm, axis=1), count_local), "batch")
        mean = first_sum / count
        centered = pre_norm - mean[:, None]
        var = lax.psum(jnp.sum(valid_row * centered * centered, axis=1), "batch") / count
        inv_std = lax.rsqrt(var + EPS)
        zhat = (pre_norm - mean[:, None]) * inv_std[:, None]
        drive = gains[layer_no][:, None] * zhat + (shifts[layer_no] + biases[layer_no])[:, None]
        drive_time = to_time(drive)
        decay_wide = jnp.tile(decays[layer_no], clips)
        start_state = jnp.zeros((clips * width,), jnp.float32)
        _, states = lax.scan(
            partial(recur_step, decay_wide), start_state, (drive_time, valid_time), unroll=8
        )
        saved.append((gathered, zhat, inv_std, drive_time, states, count))
        layer_in = layer_in + valid_row * from_time(states)
    upstream = grad_out
    grad_parts = [None] * LAYERS
    for layer_no in range(LAYERS - 1, -1, -1):
        gathered, zhat, inv_std, drive_time, states, count = saved[layer_no]
        decay_wide = jnp.tile(decays[layer_no], clips)
        gain = gains[layer_no]
        previous = jnp.concatenate([jnp.zeros_like(states[:1]), states[:-1]], axis=0)
        pre_time = drive_time + decay_wide[None, :] * previous
        grad_state = to_time(valid_row * upstream)
        start_carry = jnp.zeros((clips * width,), jnp.float32)
        _, grad_pre_time = lax.scan(
            partial(back_step, decay_wide),
            start_carry,
            (grad_state, valid_time, pre_time),
            reverse=True,
            unroll=8,
        )
        decay_local = jnp.sum(
            jnp.sum(grad_pre_time * previous, axis=0).reshape(clips, width), axis=0
        )
        grad_pre = from_time(grad_pre_time)
        gain_local = jnp.sum(grad_pre * zhat, axis=1)
        shift_local = jnp.sum(grad_pre, axis=1)
        grad_gain, grad_shift, grad_decay = lax.psum(
            (gain_local, shift_local, decay_local), "batch"
        )
        grad_pre_norm = (gain * inv_std)[:, None] * (
            grad_pre - valid_row * (grad_shift[:, None] + zhat * grad_gain[:, None]) / count
        )
        weight_local = weight_columns(grad_pre_norm, gathered)
        input_terms = jnp.einsum("jk,jf->kf", weights[layer_no], grad_pre_norm, precision=HIGH)
        input_grad = lax.psum_scatter(input_terms, "neuron", scatter_dimension=0, tiled=True)
        grad_weight = lax.psum(weight_local, "batch")
        upstream = upstream + input_grad
        grad_parts[layer_no] = (grad_weight, grad_gain, grad_shift, grad_decay)
    grad_weights = jnp.stack([grad_parts[layer_no][0] for layer_no in range(LAYERS)])
    grad_gains = jnp.stack([grad_parts[layer_no][1] for layer_no in range(LAYERS)])
    grad_shifts = jnp.stack([grad_parts[layer_no][2] for layer_no in range(LAYERS)])
    grad_decays = jnp.stack([grad_parts[layer_no][3] for layer_no in range(LAYERS)])
    return (layer_in, upstream, grad_weights, grad_gains, grad_shifts, grad_decays, grad_shifts)


def solution(mesh):
    if (mesh.shape["batch"], mesh.shape["neuron"]) == (4, 8):
        cut = Mesh(mesh.devices.reshape(2, 2, 2, 2, 2), ("y", "x", "h", "l", "c"))
        batch, neuron, body = ("y", "x"), ("h", "l", "c"), half_features
    else:
        cut, batch, neuron, body = mesh, "batch", "neuron", split_features
    in_specs = (
        P(neuron, batch),
        P(None, neuron, None),
        P(None, neuron),
        P(None, neuron),
        P(None, neuron),
        P(None, neuron),
        P(batch),
        P(batch, None),
        P(neuron, batch),
    )
    out_specs = (
        P(neuron, batch),
        P(neuron, batch),
        P(None, neuron, None),
        P(None, neuron),
        P(None, neuron),
        P(None, neuron),
        P(None, neuron),
    )
    return jax.shard_map(
        body, mesh=cut, in_specs=in_specs, out_specs=out_specs, check_vma=False
    )
```

```python
from functools import partial
import math

import jax
import jax.numpy as jnp
from jax import lax
from jax.experimental import pallas as pl
from jax.experimental.pallas import tpu as pltpu
from jax.sharding import Mesh, PartitionSpec as P

LAYERS = 2
EPS = 1e-05
HIGH = lax.Precision.HIGHEST
ROOT_TWO = math.sqrt(2.0)
ROOT_TWO_PI = math.sqrt(2.0 * math.pi)
F32 = jnp.float32
BF16 = jnp.bfloat16
LANES = 128
VMEM_LIMIT = 60 * 1024 * 1024
SMEM_SPEC = pl.BlockSpec(memory_space=pltpu.SMEM)
VMEM_SPEC = pl.BlockSpec(memory_space=pltpu.VMEM)


FLIP2 = [(0, 1), (1, 0)]
DIAGONAL = [(0, 3), (1, 2), (2, 1), (3, 0)]


def swap_half(array):
    return lax.ppermute(array, "l", FLIP2)


def after(value, *others):
    return lax.optimization_barrier((value, others))[0]


def split(value):
    high = value.astype(BF16)
    return high, (value - high.astype(F32)).astype(BF16)


def dot(a, b, dims):
    return lax.dot_general(a, b, (dims, ((), ())), preferred_element_type=F32)


NT = ((1,), (1,))
NN = ((1,), (0,))


def call(body, out_shape, **kwargs):
    in_hbm = lambda a: pltpu.HBM(a.shape, a.dtype)
    return pl.pallas_call(
        body,
        out_shape=jax.tree.map(in_hbm, out_shape),
        compiler_params=pltpu.CompilerParams(vmem_limit_bytes=VMEM_LIMIT),
        **kwargs,
    )


def cost(flops, byte_count):
    return pl.CostEstimate(flops=int(flops) // 64, bytes_accessed=int(byte_count) // 64, transcendentals=0)


def pack_body(frames, place_ref, in_ref, near_ref, far_ref, turned):
    slots = in_ref.shape[1]
    for start in range(0, slots, LANES):
        turned[start : start + LANES, :] = in_ref[:, start : start + LANES].T
    for rel in range(4):
        first = pl.multiple_of(place_ref[rel] * frames, 8)
        out = (near_ref, far_ref)[rel // 2]
        out[(rel % 2) * frames : (rel % 2 + 1) * frames, :] = turned[pl.ds(first, frames), :]


def pack(place, array, frames):
    width, slots = array.shape
    out = jax.ShapeDtypeStruct((2 * frames, width), F32)
    return call(
        partial(pack_body, frames),
        grid=(1,),
        out_shape=[out, out],
        in_specs=[SMEM_SPEC, pl.BlockSpec((width, slots), lambda i: (0, 0))],
        out_specs=[pl.BlockSpec(out.shape, lambda i: (0, 0))] * 2,
        scratch_shapes=[pltpu.VMEM((slots, width), F32)],
        cost_estimate=cost(0, 8 * width * slots),
        name="pack",
    )(place, array)


def part_spec(part, frames):
    array, i = part
    if i is None:
        return pl.BlockSpec(array.shape, lambda *_: (0,) * array.ndim)
    return pl.BlockSpec((frames, array.shape[1]), lambda *_: (i, 0))


def arrays_of(parts):
    return [array for array, _ in parts]


def unpack_body(frames, place_ref, *refs):
    ins, out_ref, turned = refs[:4], refs[4], refs[5]
    slots = out_ref.shape[1]
    for rel in range(4):
        first = pl.multiple_of(place_ref[rel] * frames, 8)
        turned[pl.ds(first, frames), :] = ins[rel][...]
    for start in range(0, slots, LANES):
        out_ref[:, start : start + LANES] = turned[start : start + LANES, :].T


def unpack(place, parts, frames):
    width = parts[0][0].shape[1]
    slots = 4 * frames
    return call(
        partial(unpack_body, frames),
        grid=(1,),
        out_shape=jax.ShapeDtypeStruct((width, slots), F32),
        in_specs=[SMEM_SPEC] + [part_spec(part, frames) for part in parts],
        out_specs=pl.BlockSpec((width, slots), lambda i: (0, 0)),
        scratch_shapes=[pltpu.VMEM((slots, width), F32)],
        cost_estimate=cost(0, 8 * width * slots),
        name="unpack",
    )(place, *arrays_of(parts))


def merge_body(kept_ref, come_ref, out_ref):
    frames, columns = kept_ref.shape
    width = columns // 2
    for i in range(2):
        some = slice(i * width, (i + 1) * width)
        out_ref[i * frames : (i + 1) * frames, :] = kept_ref[:, some] + come_ref[:, some]


def merge(kept, half, come):
    frames, columns = come.shape
    return call(
        merge_body,
        grid=(1,),
        out_shape=jax.ShapeDtypeStruct((2 * frames, columns // 2), F32),
        in_specs=[
            pl.BlockSpec((frames, columns), lambda i: (0, half)),
            pl.BlockSpec((frames, columns), lambda i: (0, 0)),
        ],
        out_specs=pl.BlockSpec((2 * frames, columns // 2), lambda i: (0, 0)),
        cost_estimate=cost(0, 12 * frames * columns),
        name="merge",
    )(kept, come)


def spread_of(parts, width):
    spots, row, column = [], 0, 0
    for array, _ in parts:
        spots.append((row, column))
        if array.shape[1] == width:
            column += width
        else:
            row += array.shape[0]
    return spots


def project_body(n_parts, spots, with_acc, with_stats, with_params, flat, cols_ref, place_ref, *refs):
    del cols_ref
    parts, refs = refs[:n_parts], refs[n_parts:]
    weights, refs = refs[:4], refs[4:]
    if with_acc:
        acc_ref, refs = refs[0], refs[1:]
    if with_stats:
        valid_ref, refs = refs[0], refs[1:]
    if with_params:
        params_ref, refs = refs[0], refs[1:]
    out_ref, refs = refs[0], refs[1:]
    if with_stats:
        stats_ref, refs = refs[0], refs[1:]
    if flat:
        flat_ref, refs = refs[0], refs[1:]
    x_high, x_low = refs
    step = pl.program_id(0)
    width = x_high.shape[2]

    @pl.when(step == 0)
    def _():
        for (row, column), part in zip(spots, parts):
            rows, columns = part.shape
            for start in range(0, columns, width):
                rel = (column + start) // width
                high, low = split(part[:, start : start + width])
                x_high[rel, row : row + rows, :] = high
                x_low[rel, row : row + rows, :] = low
            if flat:
                flat_ref[row : row + rows, column : column + columns] = part[...]
        if with_acc:
            out_ref[...] = acc_ref[...]
        else:
            out_ref[...] = jnp.zeros_like(out_ref)

    stacked = jnp.concatenate([x_high[step], x_low[step], x_high[step]], axis=1)
    for block in range(4):
        w_high, w_low = split(weights[block][...].reshape(width, width))
        columns = slice(block * width, (block + 1) * width)
        out_ref[:, columns] += dot(stacked, jnp.concatenate([w_high, w_high, w_low], axis=1), NT)

    if with_stats:

        @pl.when(step == pl.num_programs(0) - 1)
        def _():
            valid = valid_ref[...]
            own = jnp.sum(valid, axis=0, keepdims=True)
            per = width // LANES
            for row in range(out_ref.shape[1] // LANES):
                z = out_ref[:, row * LANES : (row + 1) * LANES]
                total = jnp.sum(valid * z, axis=0, keepdims=True)
                centred = valid * (z - total / own)
                squares = jnp.sum(centred * centred, axis=0, keepdims=True)
                at = place_ref[row // per] * per + row % per
                stats_ref[0, pl.ds(at, 1), :] = total
                stats_ref[1, pl.ds(at, 1), :] = squares
                stats_ref[2, pl.ds(at, 1), :] = own
            if with_params:
                rest = params_ref.shape[0] - 8
                stats_ref[3] = params_ref[:8, :]
                stats_ref[4] = jnp.zeros_like(stats_ref[4])
                stats_ref[4, :rest, :] = params_ref[8:, :]


def weight_specs(weights, layer, pairs=2):
    specs = []
    for weight in weights:
        width = weight.shape[-2]
        if weight.ndim == 3:
            specs.append(
                pl.BlockSpec((1, width, pairs * width), lambda s, cols, *_: (layer, 0, cols[s]))
            )
        else:
            specs.append(pl.BlockSpec((width, pairs * width), lambda s, cols, *_: (0, cols[s])))
    return specs


def project(
    columns, place, frames, parts, weights, layer, acc=None, valid=None, params=None, flat=False
):
    width = weights[0].shape[-2]
    full = pl.BlockSpec(memory_space=pltpu.VMEM)
    in_specs = [part_spec(part, frames) for part in parts]
    in_specs += weight_specs(weights, layer, 1)
    operands = arrays_of(parts) + list(weights)
    array = jax.ShapeDtypeStruct((frames, 4 * width), F32)
    array_spec = pl.BlockSpec((frames, 4 * width), lambda s, cols, place: (0, 0))
    out_shape, out_specs = [array], [array_spec]
    if acc is not None:
        in_specs.append(full)
        operands.append(acc)
    if valid is not None:
        in_specs.append(full)
        operands.append(valid)
        stats = (3 if params is None else 5, 4 * width // LANES, LANES)
        out_shape.append(jax.ShapeDtypeStruct(stats, F32))
        out_specs.append(pl.BlockSpec(stats, lambda s, cols, place: (0, 0, 0)))
    if params is not None:
        in_specs.append(full)
        operands.append(params)
    if flat:
        out_shape.append(array)
        out_specs.append(array_spec)
    return call(
        partial(
            project_body,
            len(parts),
            spread_of(parts, width),
            acc is not None,
            valid is not None,
            params is not None,
            flat,
        ),
        grid_spec=pltpu.PrefetchScalarGridSpec(
            num_scalar_prefetch=2,
            grid=(4,),
            in_specs=in_specs,
            out_specs=out_specs,
            scratch_shapes=[pltpu.VMEM((4, frames, width), BF16)] * 2,
        ),
        out_shape=out_shape,
        cost_estimate=cost(2 * 3 * frames * 16 * width * width, 4 * 16 * width * width),
        name="project",
    )(columns, place, *operands)


def to_relative(place_ref, spread, rows_ref, value, slot):
    per = value.shape[0] // 4
    spread[...] = value
    for rel in range(4):
        first = place_ref[rel] * per
        for row in range(per):
            rows_ref[slot, rel * per + row : rel * per + row + 1, :] = spread[
                pl.ds(first + row, 1), :
            ]


def tree(values):
    while len(values) > 1:
        values = [a + b for a, b in zip(values[::2], values[1::2])]
    return values[0]


def norm_terms(stats_ref):
    step = stats_ref.shape[0] // 16
    each = [[stats_ref[i] for i in range(slot, stats_ref.shape[0], step)] for slot in range(3)]
    totals, squares, owns = each
    count = tree(owns)
    mean = tree(totals) / count
    away = [total / own - mean for total, own in zip(totals, owns)]
    spread = tree([s + n * a * a for s, n, a in zip(squares, owns, away)])
    return count, mean, lax.rsqrt(spread / count + EPS)


def recur_body(n_parts, spots, last, layer, spread_params, place_ref, gate_ref, z_ref, stats_ref, params_ref, valid_ref, *refs):
    parts, refs = refs[:n_parts], refs[n_parts:]
    outs, refs = refs[: 1 + last], refs[1 + last :]
    if spread_params:
        state_ref, slope_ref, params_out, rows, spread, drive_s, state_s, slope_s = refs
    else:
        state_ref, slope_ref, rows, spread, drive_s, state_s, slope_s = refs
    frames = z_ref.shape[0]
    blocks = z_ref.shape[1] // LANES
    per = blocks // 4
    if spread_params:
        for rel in range(4):
            first = place_ref[rel] * (stats_ref.shape[0] // 16)
            for row in range(LAYERS * 3 * per):
                params_out[row // per, rel * per + row % per : rel * per + row % per + 1, :] = (
                    stats_ref[first + 3 + row // 8, row % 8 : row % 8 + 1, :]
                )
        params = [params_out[3 * layer + i] for i in range(3)]
    else:
        params = [params_ref[3 * layer + i] for i in range(3)]
    _, mean, inv_std = norm_terms(stats_ref)
    to_relative(place_ref, spread, rows, mean, 0)
    to_relative(place_ref, spread, rows, inv_std, 1)
    rows[1] = rows[1] * params[0]
    rows[2] = params[1]
    decay = params[2]
    for row in range(blocks):
        z = z_ref[:, row * LANES : (row + 1) * LANES]
        drive_s[row * frames : (row + 1) * frames, :] = (
            z - rows[0, row : row + 1, :]
        ) * rows[1, row : row + 1, :] + rows[2, row : row + 1, :]

    def step(t, state):
        at = pl.ds(t, blocks, stride=frames)
        pre = drive_s[at, :] + decay * state
        half = 0.5 + 0.5 * lax.erf(pre * (1.0 / ROOT_TWO))
        gate = gate_ref[t] > 0.0
        slope = half + pre * jnp.exp(-0.5 * pre * pre) * (1.0 / ROOT_TWO_PI)
        state = jnp.where(gate, pre * half, state)
        state_s[at, :] = state
        slope_s[at, :] = jnp.where(gate, slope, 0.0)
        return state

    lax.fori_loop(0, frames, step, jnp.zeros((blocks, LANES), F32), unroll=8)
    valid = valid_ref[...]
    for row in range(blocks):
        lanes = slice(row * LANES, (row + 1) * LANES)
        state = state_s[row * frames : (row + 1) * frames, :]
        state_ref[:, lanes] = state
        slope_ref[:, lanes] = slope_s[row * frames : (row + 1) * frames, :]
        for (top, column), part in zip(spots, parts):
            if column <= row * LANES < column + part.shape[1]:
                x = part[:, row * LANES - column : (row + 1) * LANES - column]
                some = slice(top, top + part.shape[0])
                value = x + valid[some] * state[some]
                if last:
                    rel, at = divmod(row * LANES, outs[0].shape[1])
                    base = (rel % 2) * frames + top
                    outs[rel // 2][base : base + part.shape[0], at : at + LANES] = value
                else:
                    outs[0][top : top + part.shape[0], lanes] = value


def recur(layer, place, gate, z, stats, params, valid, parts, last):
    frames, features = z.shape
    width = features // 4
    blocks = features // LANES
    whole = lambda array: pl.BlockSpec(array.shape, lambda i: (0,) * array.ndim)
    full = jax.ShapeDtypeStruct((frames, features), F32)
    outs = [jax.ShapeDtypeStruct((2 * frames, width), F32)] * 2 if last else [full]
    out_shape = outs + [full, full]
    spread_params = params is None
    if spread_params:
        out_shape.append(jax.ShapeDtypeStruct((3 * LAYERS, blocks, LANES), F32))
        params = valid
    return call(
        partial(recur_body, len(parts), spread_of(parts, width), last, layer, spread_params),
        grid=(1,),
        in_specs=[SMEM_SPEC, SMEM_SPEC]
        + [whole(a) for a in (z, stats, params, valid)]
        + [part_spec(part, frames) for part in parts],
        out_specs=[whole(s) for s in out_shape],
        out_shape=out_shape,
        scratch_shapes=[
            pltpu.VMEM((3, blocks, LANES), F32),
            pltpu.VMEM((blocks, LANES), F32),
        ]
        + [pltpu.VMEM((blocks * frames, LANES), F32)] * 3,
        cost_estimate=cost(100 * frames * features, 20 * frames * features),
        name="recur",
    )(place, gate, z, stats, params, valid, *arrays_of(parts))


def back_body(n_parts, spots, n_state, layer, place_ref, gate_ref, z_ref, stats_ref, params_ref, *refs):
    parts, refs = refs[:n_parts], refs[n_parts:]
    states, refs = refs[:n_state], refs[n_state:]
    slopes, refs = refs[:n_state], refs[n_state:]
    grad_ref, sums_ref, rows, spread, up_s, state_s, slope_s = refs
    frames = z_ref.shape[0]
    blocks = z_ref.shape[1] // LANES
    tall = frames + 8
    _, mean, inv_std = norm_terms(stats_ref)
    to_relative(place_ref, spread, rows, mean, 0)
    to_relative(place_ref, spread, rows, inv_std, 1)
    for row in range(blocks):
        lanes = slice(row * LANES, (row + 1) * LANES)
        base = row * frames
        up = None
        for (top, column), part in zip(spots, parts):
            if column <= row * LANES < column + part.shape[1] and part.shape[0] == frames:
                value = part[:, row * LANES - column : (row + 1) * LANES - column]
                up = value if up is None else up + value
        up_s[base : base + frames, :] = up
        state_s[row * tall : row * tall + 8, :] = jnp.zeros((8, LANES), F32)
        first = 0
        for state, slope in zip(states, slopes):
            some = state.shape[0]
            at = row * tall + 8 + first
            state_s[at : at + some, :] = state[:, lanes]
            slope_s[base + first : base + first + some, :] = slope[:, lanes]
            first += some
    decay = params_ref[3 * layer + 2]

    def step(i, carry):
        t = frames - 1 - i
        at = pl.ds(t, blocks, stride=frames)
        slope = slope_s[at, :]
        gate = gate_ref[t]
        total = gate * up_s[at, :] + carry
        up_s[at, :] = total * slope
        return total * (slope * decay + (1.0 - gate))

    lax.fori_loop(0, frames, step, jnp.zeros((blocks, LANES), F32), unroll=8)
    per = blocks // 4
    for row in range(blocks):
        lanes = slice(row * LANES, (row + 1) * LANES)
        base = row * frames
        grad = up_s[base : base + frames, :]
        grad_ref[:, lanes] = grad
        zhat = (z_ref[:, lanes] - rows[0, row : row + 1, :]) * rows[1, row : row + 1, :]
        before = state_s[row * tall + 7 : row * tall + 7 + frames, :]
        at = place_ref[row // per] * per + row % per
        for slot, value in enumerate((grad * zhat, grad, grad * before)):
            sums_ref[slot, pl.ds(at, 1), :] = jnp.sum(value, axis=0, keepdims=True)


def spots_of_sum(parts, width):
    spots, column = [], 0
    for array, _ in parts:
        spots.append((0, column % (4 * width)))
        column += array.shape[1]
    return spots


def back(layer, place, gate, z, stats, params, ups, states, slopes):
    frames, features = z.shape
    width = features // 4
    blocks = features // LANES
    whole = lambda array: pl.BlockSpec(array.shape, lambda i: (0,) * array.ndim)
    out_shape = [
        jax.ShapeDtypeStruct((frames, features), F32),
        jax.ShapeDtypeStruct((3, blocks, LANES), F32),
    ]
    return call(
        partial(back_body, len(ups), spots_of_sum(ups, width), len(states), layer),
        grid=(1,),
        in_specs=[SMEM_SPEC] * 2
        + [whole(a) for a in (z, stats, params)]
        + [part_spec(up, frames) for up in ups]
        + [whole(a) for a in (*states, *slopes)],
        out_specs=[whole(a) for a in out_shape],
        out_shape=out_shape,
        scratch_shapes=[
            pltpu.VMEM((2, blocks, LANES), F32),
            pltpu.VMEM((blocks, LANES), F32),
            pltpu.VMEM((blocks * frames, LANES), F32),
            pltpu.VMEM((blocks * (frames + 8), LANES), F32),
            pltpu.VMEM((blocks * frames, LANES), F32),
        ],
        cost_estimate=cost(30 * frames * features, 20 * frames * features),
        name="back",
    )(place, gate, z, stats, params, *arrays_of(ups), *states, *slopes)


def input_terms(high_s, low_s, weights):
    width = high_s.shape[2]
    left, right = [], []
    for block, weight in enumerate(weights):
        w_high, w_low = split(weight[...].reshape(width, 2 * width))
        left += [high_s[block], low_s[block], high_s[block]]
        right += [w_high, w_high, w_low]
    return dot(jnp.concatenate(left, axis=1), jnp.concatenate(right, axis=0), NN)


def norm_back_body(split_terms, layer, cols_ref, place_ref, grad_ref, z_ref, params_ref, valid_ref, stats_ref, sums_ref, *refs):
    del cols_ref
    weights, refs = refs[:4], refs[4:]
    if split_terms:
        out_ref, leave_ref, near_term_ref, far_term_ref, sums_out_ref, *refs = refs
        term_refs, starts = (far_term_ref, near_term_ref), (0, 0)
    else:
        out_ref, leave_ref, term_ref, sums_out_ref, *refs = refs
        term_refs, starts = (term_ref, term_ref), (2 * grad_ref.shape[1] // 4, 0)
    rows, spread, high_s, low_s = refs
    blocks = z_ref.shape[1] // LANES
    width = high_s.shape[2]
    per = width // LANES

    @pl.when(pl.program_id(0) == 0)
    def _():
        count, mean, inv_std = norm_terms(stats_ref)
        to_relative(place_ref, spread, rows, mean, 0)
        to_relative(place_ref, spread, rows, inv_std, 1)
        rows[2] = rows[1] * params_ref[3 * layer]
        sums = tree([sums_ref[i : i + 3] for i in range(0, sums_ref.shape[0], 3)])
        sums_out_ref[...] = sums
        to_relative(place_ref, spread, rows, sums[0] / count, 3)
        to_relative(place_ref, spread, rows, sums[1] / count, 4)
        valid = valid_ref[...]
        for row in range(blocks):
            lanes = slice(row * LANES, (row + 1) * LANES)
            one = lambda slot: rows[slot, row : row + 1, :]
            zhat = (z_ref[:, lanes] - one(0)) * one(1)
            value = one(2) * (grad_ref[:, lanes] - valid * (one(4) + zhat * one(3)))
            out_ref[:, lanes] = value
            if (row // per) % 2:
                at = (row // per // 2) * width + (row % per) * LANES
                leave_ref[:, at : at + LANES] = value
            high, low = split(value)
            inner = slice((row % per) * LANES, (row % per + 1) * LANES)
            high_s[row // per, :, inner] = high
            low_s[row // per, :, inner] = low

    value = input_terms(high_s, low_s, weights)
    for step, (term_ref, first) in enumerate(zip(term_refs, starts)):

        @pl.when(pl.program_id(0) == step)
        def _():
            for pair in range(2):
                at = pl.multiple_of(((place_ref[0] & 1) ^ pair) * width, width)
                term_ref[:, pl.ds(first + at, width)] = value[
                    :, pair * width : (pair + 1) * width
                ]


def norm_back(columns, place, grad, z, params, valid, stats, sums, weights, layer, split_terms):
    frames, features = z.shape
    width = features // 4
    blocks = features // LANES
    whole = lambda array: pl.BlockSpec(array.shape, lambda s, cols, place: (0,) * array.ndim)
    operands = [grad, z, params, valid, stats, sums]
    full = jax.ShapeDtypeStruct((frames, features), F32)
    half = jax.ShapeDtypeStruct((frames, 2 * width), F32)
    terms = [half, half] if split_terms else [full]
    out_shape = [full, half, *terms, jax.ShapeDtypeStruct((3, blocks, LANES), F32)]
    return call(
        partial(norm_back_body, split_terms, layer),
        grid_spec=pltpu.PrefetchScalarGridSpec(
            num_scalar_prefetch=2,
            grid=(2,),
            in_specs=[whole(a) for a in operands] + weight_specs(weights, layer),
            out_specs=[whole(a) for a in out_shape],
            scratch_shapes=[
                pltpu.VMEM((5, blocks, LANES), F32),
                pltpu.VMEM((blocks, LANES), F32),
                pltpu.VMEM((4, frames, width), BF16),
                pltpu.VMEM((4, frames, width), BF16),
            ],
        ),
        out_shape=out_shape,
        cost_estimate=cost(6 * frames * features * features, 4 * features * features),
        name="norm_back",
    )(columns, place, *operands, *weights)


def own_terms_body(n_ups, spots, cols_ref, place_ref, grad_ref, *refs):
    del cols_ref
    ups, refs = refs[:n_ups], refs[n_ups:]
    weights, refs = refs[:4], refs[4:]
    out_ref, high_s, low_s = refs
    width = high_s.shape[2]
    step = pl.program_id(0)

    @pl.when(step == 0)
    def _():
        for block in range(4):
            high, low = split(grad_ref[:, block * width : (block + 1) * width])
            high_s[block] = high
            low_s[block] = low

    value = input_terms(high_s, low_s, weights)
    for pair in range(2):
        at = pl.multiple_of(((place_ref[0] & 1) ^ pair) * width, width)
        out_ref[:, pl.ds(at, width)] = value[:, pair * width : (pair + 1) * width]
    for half in range(2):

        @pl.when(step == half)
        def _():
            first = 2 * half * width
            for (_, column), up in zip(spots, ups):
                low = max(column, first)
                high = min(column + up.shape[1], first + 2 * width)
                if low < high:
                    out_ref[:, low - first : high - first] += up[:, low - column : high - column]


def own_terms(columns, place, grad, ups, weights, layer):
    frames, features = grad.shape
    width = features // 4
    whole = lambda array: pl.BlockSpec(array.shape, lambda s, cols, place: (0,) * array.ndim)
    step_block = pl.BlockSpec((frames, 2 * width), lambda s, cols, place: (0, s))
    return call(
        partial(own_terms_body, len(ups), spots_of_sum(ups, width)),
        grid_spec=pltpu.PrefetchScalarGridSpec(
            num_scalar_prefetch=2,
            grid=(2,),
            in_specs=[whole(grad)]
            + [part_spec(up, frames) for up in ups]
            + weight_specs(weights, layer),
            out_specs=step_block,
            scratch_shapes=[pltpu.VMEM((4, frames, width), BF16)] * 2,
        ),
        out_shape=jax.ShapeDtypeStruct((frames, features), F32),
        cost_estimate=cost(6 * frames * features * features, 4 * features * features),
        name="own_terms",
    )(columns, place, grad, *arrays_of(ups), *weights)


def prepare_body(n_chunks, lists_ref, *refs):
    del lists_ref
    groups = []
    for _ in range(4):
        groups.append(refs[:n_chunks])
        refs = refs[n_chunks:]
    high_ref, low_ref = refs
    padded = high_ref.shape[0] // 2
    for side in range(2):

        @pl.when(pl.program_id(0) // 4 == side)
        def _():
            for clip in range(2):
                row = clip * padded
                for part in groups[2 * clip + side]:
                    rows = part.shape[0]
                    high, low = split(part[...])
                    high_ref[row : row + rows, :] = high
                    low_ref[row : row + rows, :] = low
                    row += rows
                rest = (clip + 1) * padded - row
                zeros = jnp.zeros((rest, high_ref.shape[1]), BF16)
                high_ref[row : row + rest, :] = zeros
                low_ref[row : row + rest, :] = zeros


def prepare(lists, groups):
    width = groups[0][0].shape[1] // 4
    frames = sum(part.shape[0] for part in groups[0])
    padded = -(-frames // LANES) * LANES
    in_specs = []
    for i, group in enumerate(groups):
        for part in group:
            if i % 2 == 0:
                index = lambda s, cols, flip=i // 2: (0, jnp.minimum(s, 3) ^ flip)
            else:
                index = lambda s, cols, flip=i // 2: (0, jnp.maximum(s - 4, 0) ^ flip)
            in_specs.append(pl.BlockSpec((part.shape[0], width), index))
    out = jax.ShapeDtypeStruct((2 * padded, 8 * width), BF16)
    return call(
        partial(prepare_body, len(groups[0])),
        grid_spec=pltpu.PrefetchScalarGridSpec(
            num_scalar_prefetch=1,
            grid=(8,),
            in_specs=in_specs,
            out_specs=[pl.BlockSpec((2 * padded, width), lambda s, cols: (0, cols[s]))] * 2,
        ),
        out_shape=[out, out],
        cost_estimate=cost(0, 16 * frames * 8 * width),
        name="prepare",
    )(lists, *[part for group in groups for part in group])


def product(g_high, g_low, x_high, x_low):
    return dot(g_high, x_high, NN) + (dot(g_high, x_low, NN) + dot(g_low, x_high, NN))


def weight_body(turn, place_ref, *refs):
    if turn:
        grad_ref, near_ref, x_high, x_low, kept, sent, g_high, g_low, t_high, t_low = refs

        @pl.when(pl.program_id(0) == 0)
        def _():
            frames, features = grad_ref.shape
            width = features // 4
            rows = width // 4
            padded = t_high.shape[1] // 2
            t_high[...] = jnp.zeros_like(t_high)
            t_low[...] = jnp.zeros_like(t_low)
            for clip in range(2):
                for dh in range(2):
                    if clip == 0:
                        part = grad_ref[:, 2 * dh * width : (2 * dh + 1) * width]
                    else:
                        part = near_ref[:, dh * width : (dh + 1) * width]
                    high, low = split(part.T)
                    at = (
                        slice(dh * width, (dh + 1) * width),
                        slice(clip * padded, clip * padded + frames),
                    )
                    t_high[at] = high
                    t_low[at] = low
            for group in range(8):
                first, second, dh = group // 4, group // 2 % 2, group % 2
                core = place_ref[6]
                y = place_ref[4] ^ (first * core + second * (1 - core))
                x = place_ref[5] ^ (first * (1 - core) + second * core)
                at = pl.multiple_of(dh * width + (2 * y + x) * rows, rows)
                g_high[group * rows : (group + 1) * rows, :] = t_high[pl.ds(at, rows), :]
                g_low[group * rows : (group + 1) * rows, :] = t_low[pl.ds(at, rows), :]

    else:
        g_high, g_low, x_high, x_low, kept, sent = refs
    half = g_high.shape[0] // 2
    value = product(g_high[...], g_low[...], x_high[...], x_low[...])
    kept[...] = value[:half].reshape(kept.shape)
    sent[...] = value[half:].reshape(sent.shape)


def weight_rows(half, place, grads, x_split, width):
    turn = half == 0
    whole = lambda array: pl.BlockSpec(array.shape, lambda s, place: (0,) * array.ndim)
    x_spec = pl.BlockSpec((x_split[0].shape[0], width), lambda s, place: (0, 4 * half + s))
    shape = (2, 2, width // 4, 4 * width)
    out_shape = [jax.ShapeDtypeStruct(shape, F32)] * 2
    out_specs = [pl.BlockSpec(shape[:3] + (width,), lambda s, place: (0, 0, 0, s))] * 2
    scratch = []
    if turn:
        turned = (2 * width, x_split[0].shape[0])
        out_shape += [jax.ShapeDtypeStruct(turned, BF16)] * 2
        out_specs += [whole(out_shape[-1])] * 2
        scratch = [pltpu.VMEM(turned, BF16)] * 2
    return call(
        partial(weight_body, turn),
        grid_spec=pltpu.PrefetchScalarGridSpec(
            num_scalar_prefetch=1,
            grid=(4,),
            in_specs=[whole(a) for a in grads] + [x_spec] * 2,
            out_specs=out_specs,
            scratch_shapes=scratch,
        ),
        out_shape=out_shape,
        cost_estimate=cost(12 * x_split[0].shape[0] * width * 4 * width, 4 * 8 * width * width),
        name="weight_rows",
    )(place, *grads, *x_split)


def step_body(n, *refs):
    outs = refs[2 * n :]
    column = 0
    for i in range(n):
        total = refs[2 * i][...] + refs[2 * i + 1][...]
        some = slice(column, column + total.shape[-1])
        if len(outs) == 1:
            outs[0][..., some] = total
        else:
            for j, out in enumerate(outs):
                out[..., some] = total[j]
        column += total.shape[-1]


def step_of(*pairs, cut=True):
    shape = list(pairs[0][0].shape)
    shape[-1] = sum(pair[0].shape[-1] for pair in pairs)
    out = jax.ShapeDtypeStruct(tuple(shape[1:] if cut else shape), F32)
    outs = [out, out] if cut else [out]
    whole = lambda array: pl.BlockSpec(array.shape, lambda i: (0,) * array.ndim)
    operands = [array for pair in pairs for array in pair]
    return call(
        partial(step_body, len(pairs)),
        grid=(1,),
        in_specs=[whole(a) for a in operands],
        out_specs=[whole(a) for a in outs],
        out_shape=outs,
        cost_estimate=cost(0, 4 * sum(a.size for a in operands)),
        name="reduction_step",
    )(*operands)


def plane_swap(array, step):
    pairs = []
    for i in range(8):
        over_x = (i % 2 == 0) == (step == 0)
        pairs.append((i, i ^ 2 if over_x else i ^ 4))
    return lax.ppermute(array, ("y", "x", "c"), pairs)


def plane_gather(share, *before):
    first = plane_swap(share, 0)
    second = plane_swap(share, 1)
    return [share, second, first, plane_swap(after(first, *before), 1)]


def assemble_body(groups, by_core, place_ref, *refs):
    out_ref = refs[-1]
    core = place_ref[6] if by_core else 0
    column = 0
    for group in range(groups):
        rows, columns = refs[4 * group].shape
        for i in range(4):
            first, second = i // 2, i % 2
            if by_core:
                first, second = (
                    first * core + second * (1 - core),
                    first * (1 - core) + second * core,
                )
            at = pl.multiple_of((2 * (place_ref[4] ^ first) + (place_ref[5] ^ second)) * rows, rows)
            out_ref[..., pl.ds(at, rows), column : column + columns] = refs[4 * group + i][
                ...
            ].reshape(out_ref.shape[:-2] + (rows, columns))
        column += columns


def assemble(place, groups, layer=None, onto=None, by_core=True):
    pieces = [piece for group in groups for piece in group]
    rows = pieces[0].shape[0]
    shape = (4 * rows, sum(group[0].shape[1] for group in groups))
    out_spec = pl.BlockSpec(shape, lambda i: (0, 0))
    aliases, extra, extra_specs = {}, [], []
    if layer is not None:
        out_spec = pl.BlockSpec((1, *shape), lambda i: (layer, 0, 0))
        shape = (LAYERS, *shape)
    if onto is not None:
        aliases, extra = {1 + len(pieces): 0}, [onto]
        extra_specs = [pl.BlockSpec(memory_space=pl.ANY)]
    return call(
        partial(assemble_body, len(groups), by_core),
        grid=(1,),
        out_shape=jax.ShapeDtypeStruct(shape, F32),
        in_specs=[SMEM_SPEC]
        + [pl.BlockSpec(p.shape, lambda i: (0, 0)) for p in pieces]
        + extra_specs,
        out_specs=out_spec,
        input_output_aliases=aliases,
        cost_estimate=cost(0, 8 * shape[-1] * shape[-2]),
        name="assemble",
    )(place, *pieces, *extra)


def half_features(inputs, weights, gains, shifts, decays, biases, lengths, frame_mask, grad_out):
    width, slots = inputs.shape
    clips, frames = frame_mask.shape
    depth = weights.shape[2]
    blocks = 4 * width // LANES
    y, x, h, l, c = (lax.axis_index(name) for name in ("y", "x", "h", "l", "c"))
    b = 2 * y + x
    numbers = [2 * (h ^ (rel // 2)) + (c ^ (rel % 2)) for rel in range(4)] + [y, x, c]
    place = jnp.stack(numbers).astype(jnp.int32)
    own_blocks, other_blocks = (
        jnp.stack(
            [2 * (2 * (h ^ (rel // 2)) + half) + (c ^ (rel % 2)) for rel in range(4)]
        ).astype(jnp.int32)
        for half in (l, 1 - l)
    )
    all_blocks = jnp.concatenate([own_blocks, other_blocks])
    own_columns = jnp.stack([2 * h + l, 2 * (1 - h) + l]).astype(jnp.int32)
    other_columns = jnp.stack([2 * (1 - h) + 1 - l, 2 * h + 1 - l]).astype(jnp.int32)
    rows = width // 4

    clip = 2 * h + c
    seen = lax.dynamic_index_in_dim(frame_mask, clip, 0, keepdims=False)
    length = lax.dynamic_index_in_dim(lengths, clip, 0, keepdims=False)
    moments = jnp.arange(frames, dtype=jnp.int32)
    gate = ((moments < length) & ((seen == 1) | (moments == 0))).astype(F32)
    valid = jnp.broadcast_to(gate[:, None], (frames, LANES))

    def far_share(layer):
        return lax.dynamic_slice(weights, (layer, b * rows, 0), (1, rows, depth))[0]

    def over_h(array):
        return lax.ppermute(array, "h", FLIP2)

    def over_c(array):
        return lax.ppermute(array, "c", FLIP2)

    def over_second(array):
        return plane_swap(array, 1)

    def four_of(near_rows, far_rows):
        return [
            (near_rows, 0),
            (over_c(near_rows), 1),
            (far_rows, 0),
            (over_c(far_rows), 1),
        ]

    def far_blocks(share):
        both = lax.ppermute(share, ("y", "x"), DIAGONAL)
        shares = [share, lax.ppermute(share, "x", FLIP2), lax.ppermute(share, "y", FLIP2), both]
        other = [over_c(piece) for piece in shares]
        return [assemble(place, [pieces], by_core=False) for pieces in (shares, other)]

    near = over_c(weights)
    share = far_share(0)
    close, away = pack(place, after(inputs, share), frames)
    share = over_h(share)
    away = over_h(away)
    other_close = swap_half(close)
    up_close, up_away = pack(place, after(grad_out, close), frames)
    share = after(share, up_close, valid)
    own = four_of(close, away)
    other_away = swap_half(away)
    half_weights = [[weights, near, *far_blocks(share)]]
    params = jnp.stack([gains, shifts + biases, decays], axis=1)
    own_params = params.reshape(LAYERS * 3 * width // LANES, LANES)
    params = None

    saved = []
    for layer in range(LAYERS):
        last = layer == LAYERS - 1
        flat = layer == 0
        if layer > 0:
            others = [(swap_half(array), None) for array, _ in own]
        z, *own_flat = project(
            own_blocks, place, frames, own, half_weights[layer], layer, flat=flat
        )
        if flat:
            others = four_of(other_close, after(other_away, z))
        z, stats, *other_flat = project(
            other_blocks,
            place,
            frames,
            others,
            half_weights[layer],
            layer,
            z,
            valid,
            own_params if flat else None,
            flat,
        )
        if last:
            upstream = four_of(up_close, after(up_away, z))
        if flat:
            stats = lax.all_gather(stats, ("h", "c"), tiled=True)
            share = over_h(after(far_share(1), stats))
            stats = lax.all_gather(stats, ("y", "x"), tiled=True)
        else:
            stats = lax.all_gather(stats, ("y", "x"), tiled=True)
            stats = lax.all_gather(stats, ("h", "c"), tiled=True)
        *following, states, slopes = recur(
            layer, place, gate, z, stats, params, valid, own, last
        )
        if flat:
            *following, states, slopes, params = *following, states, slopes
            groups = [own_flat, other_flat]
        else:
            groups = [arrays_of(own), arrays_of(others)]
        groups += [[over_c(after(p, z)) for p in group] for group in groups]
        x_split = prepare(all_blocks, after(groups, slopes)) if flat else None
        if flat:
            up_away = over_h(after(up_away, x_split[0], share))
            half_weights.append([weights, near, *far_blocks(after(share, slopes))])
        saved.append((groups, x_split, z, stats, states, slopes))
        own = [(array, None) for array in following]
    close, away = following
    away = over_h(away)
    output = four_of(close, away)

    ups = upstream
    results = [None] * LAYERS
    for layer in range(LAYERS - 1, -1, -1):
        groups, x_split, z, stats, states, slopes = saved[layer]
        weight = half_weights[layer]
        grad_pre, sums = back(
            layer, place, gate, z, stats, params, ups, [states], [slopes]
        )
        plane = lax.all_gather(sums, ("y", "x"), tiled=True)
        if layer == 0:
            later, go = step_of(*[(k, after(g, plane)) for k, g in zip(stay, come)])
            plane = after(plane, later)
            go = over_second(go)
        sums = lax.all_gather(plane, ("h", "c"), tiled=True)
        grad_z, leaving, *terms, sums = norm_back(
            other_columns, place, grad_pre, z, params, valid, stats, sums, weight, layer,
            layer == 0,
        )
        leaving = over_c(leaving)
        if layer > 0:
            received = [swap_half(terms[0])]
            x_split = prepare(all_blocks, after(groups, grad_z, away))
        else:
            received = [None, swap_half(terms[1])]
            later, go = step_of((later, after(go, grad_z)))
            leaving = after(leaving, later)
            later = (later, over_h(go))
        *first, g_high, g_low = weight_rows(0, place, (grad_z, leaving), x_split, width)
        turned = (g_high, g_low)
        come = [plane_swap(first[1], 0)]
        if layer == 0:
            received[0] = swap_half(after(terms[0], received[1]))
        second = weight_rows(1, place, turned, x_split, width)
        come.append(plane_swap(second[1], 0))
        stay = (first[0], second[0])
        kept = own_terms(own_columns, place, after(grad_z, second[0]), ups, weight, layer)
        ups = [(kept, None)] + [(r, None) for r in received]
        results[layer] = lax.dynamic_index_in_dim(
            sums.reshape(3, 4, width), clip, axis=1, keepdims=False
        )

    away = merge(kept, 1, received[1])
    (later,) = step_of((later[0], after(later[1], away)), cut=False)
    away = over_h(away)
    later_first, later_second = plane_swap(later, 0), plane_swap(later, 1)
    total, go = step_of((stay[0], after(come[0], later_first)), (stay[1], come[1]))
    go = over_second(go)
    later = [later, later_second, later_first, plane_swap(after(later_first, total), 1)]
    close = merge(kept, 0, after(received[0], total))
    grad_in = four_of(close, away)
    total, go = step_of((total, after(go, close, grad_in[3][0])))
    go = over_h(go)
    grad_weights = assemble(place, after([later], total), 1)
    output = unpack(place, [(after(array, grad_weights), i) for array, i in output], frames)
    grad_in = unpack(place, [(after(array, output), i) for array, i in grad_in], frames)
    (share,) = step_of((total, after(go, grad_in)), cut=False)
    grad_weights = assemble(place, [plane_gather(share)], 0, grad_weights)
    sums = jnp.stack(results)
    return (
        output,
        grad_in,
        grad_weights,
        sums[:, 0],
        sums[:, 1],
        sums[:, 2],
        sums[:, 1],
    )


def gelu_slope(value):
    return (
        0.5 * (1.0 + jax.scipy.special.erf(value / ROOT_TWO))
        + value * jnp.exp(-0.5 * value * value) / ROOT_TWO_PI
    )


def recur_step(decay, state, inputs):
    drive_t, valid_t = inputs
    pre = drive_t + decay * state
    state = state + valid_t * (jax.nn.gelu(pre, approximate=False) - state)
    return (state, state)


def back_step(decay, carry, inputs):
    upstream_t, valid_t, pre_t = inputs
    total = upstream_t + carry
    grad_pre = total * valid_t * gelu_slope(pre_t)
    carry = total * (1.0 - valid_t) + grad_pre * decay
    return (carry, grad_pre)


def add_piece(weight, piece):
    return jnp.dot(weight, piece, precision=HIGH, preferred_element_type=jnp.float32)


def weight_columns(grad_pre_norm, piece):
    return jnp.einsum("jf,kf->jk", grad_pre_norm, piece, precision=HIGH)


def split_features(inputs, weights, gains, shifts, decays, biases, lengths, frame_mask, grad_out):
    width, slots = inputs.shape
    clips, frames_len = frame_mask.shape
    frames = jnp.arange(frames_len, dtype=jnp.int32)
    valid_grid = (
        (frames[None, :] < lengths[:, None]) & ((frame_mask == 1) | (frames[None, :] == 0))
    ).astype(jnp.float32)
    valid = valid_grid.reshape(-1)
    valid_row = valid[None, :]
    valid_time = jnp.broadcast_to(valid_grid.T[:, :, None], (frames_len, clips, width)).reshape(
        frames_len, clips * width
    )
    count_local = jnp.sum(valid)

    def to_time(array):
        return jnp.transpose(array.reshape(width, clips, frames_len), (2, 1, 0)).reshape(
            frames_len, clips * width
        )

    def from_time(array):
        return jnp.transpose(array.reshape(frames_len, clips, width), (2, 1, 0)).reshape(
            width, slots
        )

    layer_in = inputs
    saved = []
    for layer_no in range(LAYERS):
        weight = weights[layer_no]
        gathered = lax.all_gather(layer_in, "neuron", axis=0, tiled=True)
        pre_norm = add_piece(weight, gathered)
        first_sum, count = lax.psum((jnp.sum(valid_row * pre_norm, axis=1), count_local), "batch")
        mean = first_sum / count
        centered = pre_norm - mean[:, None]
        var = lax.psum(jnp.sum(valid_row * centered * centered, axis=1), "batch") / count
        inv_std = lax.rsqrt(var + EPS)
        zhat = (pre_norm - mean[:, None]) * inv_std[:, None]
        drive = gains[layer_no][:, None] * zhat + (shifts[layer_no] + biases[layer_no])[:, None]
        drive_time = to_time(drive)
        decay_wide = jnp.tile(decays[layer_no], clips)
        start_state = jnp.zeros((clips * width,), jnp.float32)
        _, states = lax.scan(
            partial(recur_step, decay_wide), start_state, (drive_time, valid_time), unroll=8
        )
        saved.append((gathered, zhat, inv_std, drive_time, states, count))
        layer_in = layer_in + valid_row * from_time(states)
    upstream = grad_out
    grad_parts = [None] * LAYERS
    for layer_no in range(LAYERS - 1, -1, -1):
        gathered, zhat, inv_std, drive_time, states, count = saved[layer_no]
        decay_wide = jnp.tile(decays[layer_no], clips)
        gain = gains[layer_no]
        previous = jnp.concatenate([jnp.zeros_like(states[:1]), states[:-1]], axis=0)
        pre_time = drive_time + decay_wide[None, :] * previous
        grad_state = to_time(valid_row * upstream)
        start_carry = jnp.zeros((clips * width,), jnp.float32)
        _, grad_pre_time = lax.scan(
            partial(back_step, decay_wide),
            start_carry,
            (grad_state, valid_time, pre_time),
            reverse=True,
            unroll=8,
        )
        decay_local = jnp.sum(
            jnp.sum(grad_pre_time * previous, axis=0).reshape(clips, width), axis=0
        )
        grad_pre = from_time(grad_pre_time)
        gain_local = jnp.sum(grad_pre * zhat, axis=1)
        shift_local = jnp.sum(grad_pre, axis=1)
        grad_gain, grad_shift, grad_decay = lax.psum(
            (gain_local, shift_local, decay_local), "batch"
        )
        grad_pre_norm = (gain * inv_std)[:, None] * (
            grad_pre - valid_row * (grad_shift[:, None] + zhat * grad_gain[:, None]) / count
        )
        weight_local = weight_columns(grad_pre_norm, gathered)
        input_terms = jnp.einsum("jk,jf->kf", weights[layer_no], grad_pre_norm, precision=HIGH)
        input_grad = lax.psum_scatter(input_terms, "neuron", scatter_dimension=0, tiled=True)
        grad_weight = lax.psum(weight_local, "batch")
        upstream = upstream + input_grad
        grad_parts[layer_no] = (grad_weight, grad_gain, grad_shift, grad_decay)
    grad_weights = jnp.stack([grad_parts[layer_no][0] for layer_no in range(LAYERS)])
    grad_gains = jnp.stack([grad_parts[layer_no][1] for layer_no in range(LAYERS)])
    grad_shifts = jnp.stack([grad_parts[layer_no][2] for layer_no in range(LAYERS)])
    grad_decays = jnp.stack([grad_parts[layer_no][3] for layer_no in range(LAYERS)])
    return (layer_in, upstream, grad_weights, grad_gains, grad_shifts, grad_decays, grad_shifts)


def solution(mesh):
    if (mesh.shape["batch"], mesh.shape["neuron"]) == (4, 8):
        cut = Mesh(mesh.devices.reshape(2, 2, 2, 2, 2), ("y", "x", "h", "l", "c"))
        batch, neuron, body = ("y", "x"), ("h", "l", "c"), half_features
    else:
        cut, batch, neuron, body = mesh, "batch", "neuron", split_features
    in_specs = (
        P(neuron, batch),
        P(None, neuron, None),
        P(None, neuron),
        P(None, neuron),
        P(None, neuron),
        P(None, neuron),
        P(batch),
        P(batch, None),
        P(neuron, batch),
    )
    out_specs = (
        P(neuron, batch),
        P(neuron, batch),
        P(None, neuron, None),
        P(None, neuron),
        P(None, neuron),
        P(None, neuron),
        P(None, neuron),
    )
    return jax.shard_map(
        body, mesh=cut, in_specs=in_specs, out_specs=out_specs, check_vma=False
    )
```

```python
from functools import partial
import math

import jax
import jax.numpy as jnp
from jax import lax
from jax.experimental import pallas as pl
from jax.experimental.pallas import tpu as pltpu
from jax.sharding import Mesh, PartitionSpec as P

LAYERS = 2
EPS = 1e-05
HIGH = lax.Precision.HIGHEST
ROOT_TWO = math.sqrt(2.0)
ROOT_TWO_PI = math.sqrt(2.0 * math.pi)
F32 = jnp.float32
BF16 = jnp.bfloat16
LANES = 128
VMEM_LIMIT = 24 * 1024 * 1024
SMEM_SPEC = pl.BlockSpec(memory_space=pltpu.SMEM)
VMEM_SPEC = pl.BlockSpec(memory_space=pltpu.VMEM)


FLIP2 = [(0, 1), (1, 0)]
DIAGONAL = [(0, 3), (1, 2), (2, 1), (3, 0)]


def swap_half(array):
    return lax.ppermute(array, "l", FLIP2)


def after(value, *others):
    return lax.optimization_barrier((value, others))[0]


def split(value):
    high = value.astype(BF16)
    return high, (value - high.astype(F32)).astype(BF16)


def dot(a, b, dims):
    return lax.dot_general(a, b, (dims, ((), ())), preferred_element_type=F32)


NT = ((1,), (1,))
NN = ((1,), (0,))


def in_hbm(array):
    return pltpu.with_memory_space_constraint(array, pltpu.HBM)


def call(body, out_shape, hbm_outs=(), **kwargs):
    if hbm_outs:
        out_shape = [
            pltpu.HBM(a.shape, a.dtype) if i in hbm_outs else a for i, a in enumerate(out_shape)
        ]
    return pl.pallas_call(
        body,
        out_shape=out_shape,
        compiler_params=pltpu.CompilerParams(vmem_limit_bytes=VMEM_LIMIT),
        **kwargs,
    )


def cost(flops, byte_count):
    return pl.CostEstimate(flops=int(flops) // 64, bytes_accessed=int(byte_count) // 64, transcendentals=0)


def pack_body(frames, place_ref, in_ref, near_ref, far_ref, turned):
    slots = in_ref.shape[1]
    for start in range(0, slots, LANES):
        turned[start : start + LANES, :] = in_ref[:, start : start + LANES].T
    for rel in range(4):
        first = pl.multiple_of(place_ref[rel] * frames, 8)
        out = (near_ref, far_ref)[rel // 2]
        out[(rel % 2) * frames : (rel % 2 + 1) * frames, :] = turned[pl.ds(first, frames), :]


def pack(place, array, frames, waits=False):
    width, slots = array.shape
    out = jax.ShapeDtypeStruct((2 * frames, width), F32)
    return call(
        partial(pack_body, frames),
        grid=(1,),
        out_shape=[out, out],
        in_specs=[SMEM_SPEC, pl.BlockSpec((width, slots), lambda i: (0, 0))],
        out_specs=[pl.BlockSpec(out.shape, lambda i: (0, 0))] * 2,
        scratch_shapes=[pltpu.VMEM((slots, width), F32)],
        hbm_outs=(0, 1) if waits else (),
        cost_estimate=cost(0, 8 * width * slots),
        name="pack",
    )(place, in_hbm(array))


def part_spec(part, frames):
    array, i = part
    if i is None:
        return pl.BlockSpec(array.shape, lambda *_: (0,) * array.ndim)
    return pl.BlockSpec((frames, array.shape[1]), lambda *_: (i, 0))


def arrays_of(parts):
    return [array for array, _ in parts]


def unpack_body(frames, place_ref, *refs):
    ins, out_ref, turned = refs[:4], refs[4], refs[5]
    slots = out_ref.shape[1]
    for rel in range(4):
        first = pl.multiple_of(place_ref[rel] * frames, 8)
        turned[pl.ds(first, frames), :] = ins[rel][...]
    for start in range(0, slots, LANES):
        out_ref[:, start : start + LANES] = turned[start : start + LANES, :].T


def unpack(place, parts, frames):
    width = parts[0][0].shape[1]
    slots = 4 * frames
    return call(
        partial(unpack_body, frames),
        grid=(1,),
        out_shape=jax.ShapeDtypeStruct((width, slots), F32),
        in_specs=[SMEM_SPEC] + [part_spec(part, frames) for part in parts],
        out_specs=pl.BlockSpec((width, slots), lambda i: (0, 0)),
        scratch_shapes=[pltpu.VMEM((slots, width), F32)],
        cost_estimate=cost(0, 8 * width * slots),
        name="unpack",
    )(place, *arrays_of(parts))


def merge_body(kept_ref, come_ref, out_ref):
    frames, columns = kept_ref.shape
    width = columns // 2
    for i in range(2):
        some = slice(i * width, (i + 1) * width)
        out_ref[i * frames : (i + 1) * frames, :] = kept_ref[:, some] + come_ref[:, some]


def merge(kept, half, come):
    frames, columns = come.shape
    return call(
        merge_body,
        grid=(1,),
        out_shape=jax.ShapeDtypeStruct((2 * frames, columns // 2), F32),
        in_specs=[
            pl.BlockSpec((frames, columns), lambda i: (0, half)),
            pl.BlockSpec((frames, columns), lambda i: (0, 0)),
        ],
        out_specs=pl.BlockSpec((2 * frames, columns // 2), lambda i: (0, 0)),
        cost_estimate=cost(0, 12 * frames * columns),
        name="merge",
    )(kept, come)


def spread_of(parts, width):
    spots, row, column = [], 0, 0
    for array, _ in parts:
        spots.append((row, column))
        if array.shape[1] == width:
            column += width
        else:
            row += array.shape[0]
    return spots


def project_body(n_parts, spots, with_acc, with_stats, with_params, flat, cols_ref, place_ref, *refs):
    del cols_ref
    parts, refs = refs[:n_parts], refs[n_parts:]
    weights, refs = refs[:4], refs[4:]
    if with_acc:
        acc_ref, refs = refs[0], refs[1:]
    if with_stats:
        valid_ref, refs = refs[0], refs[1:]
    if with_params:
        params_ref, refs = refs[0], refs[1:]
    out_ref, refs = refs[0], refs[1:]
    if with_stats:
        stats_ref, refs = refs[0], refs[1:]
    if flat:
        flat_ref, refs = refs[0], refs[1:]
    x_high, x_low = refs
    step = pl.program_id(0)
    width = x_high.shape[2]

    @pl.when(step == 0)
    def _():
        for (row, column), part in zip(spots, parts):
            rows, columns = part.shape
            for start in range(0, columns, width):
                rel = (column + start) // width
                high, low = split(part[:, start : start + width])
                x_high[rel, row : row + rows, :] = high
                x_low[rel, row : row + rows, :] = low
            if flat:
                flat_ref[row : row + rows, column : column + columns] = part[...]
        if with_acc:
            out_ref[...] = acc_ref[...]
        else:
            out_ref[...] = jnp.zeros_like(out_ref)

    stacked = jnp.concatenate([x_high[step], x_low[step], x_high[step]], axis=1)
    for block in range(4):
        w_high, w_low = split(weights[block][...].reshape(width, width))
        columns = slice(block * width, (block + 1) * width)
        out_ref[:, columns] += dot(stacked, jnp.concatenate([w_high, w_high, w_low], axis=1), NT)

    if with_stats:

        @pl.when(step == pl.num_programs(0) - 1)
        def _():
            valid = valid_ref[...]
            own = jnp.sum(valid, axis=0, keepdims=True)
            per = width // LANES
            for row in range(out_ref.shape[1] // LANES):
                z = out_ref[:, row * LANES : (row + 1) * LANES]
                total = jnp.sum(valid * z, axis=0, keepdims=True)
                centred = valid * (z - total / own)
                squares = jnp.sum(centred * centred, axis=0, keepdims=True)
                at = place_ref[row // per] * per + row % per
                stats_ref[0, pl.ds(at, 1), :] = total
                stats_ref[1, pl.ds(at, 1), :] = squares
                stats_ref[2, pl.ds(at, 1), :] = own
            if with_params:
                rest = params_ref.shape[0] - 8
                stats_ref[3] = params_ref[:8, :]
                stats_ref[4] = jnp.zeros_like(stats_ref[4])
                stats_ref[4, :rest, :] = params_ref[8:, :]


def weight_specs(weights, layer, pairs=2):
    specs = []
    for weight in weights:
        width = weight.shape[-2]
        if weight.ndim == 3:
            specs.append(
                pl.BlockSpec((1, width, pairs * width), lambda s, cols, *_: (layer, 0, cols[s]))
            )
        else:
            specs.append(pl.BlockSpec((width, pairs * width), lambda s, cols, *_: (0, cols[s])))
    return specs


def project(
    columns, place, frames, parts, weights, layer, acc=None, valid=None, params=None, flat=False
):
    width = weights[0].shape[-2]
    full = pl.BlockSpec(memory_space=pltpu.VMEM)
    in_specs = [part_spec(part, frames) for part in parts]
    in_specs += weight_specs(weights, layer, 1)
    operands = arrays_of(parts) + [in_hbm(w) for w in weights]
    array = jax.ShapeDtypeStruct((frames, 4 * width), F32)
    array_spec = pl.BlockSpec((frames, 4 * width), lambda s, cols, place: (0, 0))
    out_shape, out_specs = [array], [array_spec]
    if acc is not None:
        in_specs.append(full)
        operands.append(acc)
    if valid is not None:
        in_specs.append(full)
        operands.append(valid)
        stats = (3 if params is None else 5, 4 * width // LANES, LANES)
        out_shape.append(jax.ShapeDtypeStruct(stats, F32))
        out_specs.append(pl.BlockSpec(stats, lambda s, cols, place: (0, 0, 0)))
    if params is not None:
        in_specs.append(full)
        operands.append(params)
    if flat:
        out_shape.append(array)
        out_specs.append(array_spec)
    return call(
        partial(
            project_body,
            len(parts),
            spread_of(parts, width),
            acc is not None,
            valid is not None,
            params is not None,
            flat,
        ),
        grid_spec=pltpu.PrefetchScalarGridSpec(
            num_scalar_prefetch=2,
            grid=(4,),
            in_specs=in_specs,
            out_specs=out_specs,
            scratch_shapes=[pltpu.VMEM((4, frames, width), BF16)] * 2,
        ),
        out_shape=out_shape,
        hbm_outs=((1,) if valid is None else (0, 2)) if flat else (),
        cost_estimate=cost(2 * 3 * frames * 16 * width * width, 4 * 16 * width * width),
        name="project",
    )(columns, place, *operands)


def to_relative(place_ref, spread, rows_ref, value, slot):
    per = value.shape[0] // 4
    spread[...] = value
    for rel in range(4):
        first = place_ref[rel] * per
        for row in range(per):
            rows_ref[slot, rel * per + row : rel * per + row + 1, :] = spread[
                pl.ds(first + row, 1), :
            ]


def tree(values):
    while len(values) > 1:
        values = [a + b for a, b in zip(values[::2], values[1::2])]
    return values[0]


def norm_terms(stats_ref):
    step = stats_ref.shape[0] // 16
    each = [[stats_ref[i] for i in range(slot, stats_ref.shape[0], step)] for slot in range(3)]
    totals, squares, owns = each
    count = tree(owns)
    mean = tree(totals) / count
    away = [total / own - mean for total, own in zip(totals, owns)]
    spread = tree([s + n * a * a for s, n, a in zip(squares, owns, away)])
    return count, mean, lax.rsqrt(spread / count + EPS)


def recur_body(n_parts, spots, last, layer, spread_params, place_ref, gate_ref, z_ref, stats_ref, params_ref, valid_ref, *refs):
    parts, refs = refs[:n_parts], refs[n_parts:]
    outs, refs = refs[: 1 + last], refs[1 + last :]
    if spread_params:
        state_ref, slope_ref, params_out, rows, spread, drive_s, state_s, slope_s = refs
    else:
        state_ref, slope_ref, rows, spread, drive_s, state_s, slope_s = refs
    frames = z_ref.shape[0]
    blocks = z_ref.shape[1] // LANES
    per = blocks // 4
    if spread_params:
        for rel in range(4):
            first = place_ref[rel] * (stats_ref.shape[0] // 16)
            for row in range(LAYERS * 3 * per):
                params_out[row // per, rel * per + row % per : rel * per + row % per + 1, :] = (
                    stats_ref[first + 3 + row // 8, row % 8 : row % 8 + 1, :]
                )
        params = [params_out[3 * layer + i] for i in range(3)]
    else:
        params = [params_ref[3 * layer + i] for i in range(3)]
    _, mean, inv_std = norm_terms(stats_ref)
    to_relative(place_ref, spread, rows, mean, 0)
    to_relative(place_ref, spread, rows, inv_std, 1)
    rows[1] = rows[1] * params[0]
    rows[2] = params[1]
    decay = params[2]
    for row in range(blocks):
        z = z_ref[:, row * LANES : (row + 1) * LANES]
        drive_s[row * frames : (row + 1) * frames, :] = (
            z - rows[0, row : row + 1, :]
        ) * rows[1, row : row + 1, :] + rows[2, row : row + 1, :]

    def step(t, state):
        at = pl.ds(t, blocks, stride=frames)
        pre = drive_s[at, :] + decay * state
        half = 0.5 + 0.5 * lax.erf(pre * (1.0 / ROOT_TWO))
        gate = gate_ref[t] > 0.0
        slope = half + pre * jnp.exp(-0.5 * pre * pre) * (1.0 / ROOT_TWO_PI)
        state = jnp.where(gate, pre * half, state)
        state_s[at, :] = state
        slope_s[at, :] = jnp.where(gate, slope, 0.0)
        return state

    lax.fori_loop(0, frames, step, jnp.zeros((blocks, LANES), F32), unroll=8)
    valid = valid_ref[...]
    for row in range(blocks):
        lanes = slice(row * LANES, (row + 1) * LANES)
        state = state_s[row * frames : (row + 1) * frames, :]
        state_ref[:, lanes] = state
        slope_ref[:, lanes] = slope_s[row * frames : (row + 1) * frames, :]
        for (top, column), part in zip(spots, parts):
            if column <= row * LANES < column + part.shape[1]:
                x = part[:, row * LANES - column : (row + 1) * LANES - column]
                some = slice(top, top + part.shape[0])
                value = x + valid[some] * state[some]
                if last:
                    rel, at = divmod(row * LANES, outs[0].shape[1])
                    base = (rel % 2) * frames + top
                    outs[rel // 2][base : base + part.shape[0], at : at + LANES] = value
                else:
                    outs[0][top : top + part.shape[0], lanes] = value


def recur(layer, place, gate, z, stats, params, valid, parts, last):
    frames, features = z.shape
    width = features // 4
    blocks = features // LANES
    whole = lambda array: pl.BlockSpec(array.shape, lambda i: (0,) * array.ndim)
    full = jax.ShapeDtypeStruct((frames, features), F32)
    outs = [jax.ShapeDtypeStruct((2 * frames, width), F32)] * 2 if last else [full]
    out_shape = outs + [full, full]
    spread_params = params is None
    if spread_params:
        out_shape.append(jax.ShapeDtypeStruct((3 * LAYERS, blocks, LANES), F32))
        params = valid
    return call(
        partial(recur_body, len(parts), spread_of(parts, width), last, layer, spread_params),
        grid=(1,),
        in_specs=[SMEM_SPEC, SMEM_SPEC]
        + [whole(a) for a in (z, stats, params, valid)]
        + [part_spec(part, frames) for part in parts],
        out_specs=[whole(s) for s in out_shape],
        out_shape=out_shape,
        scratch_shapes=[
            pltpu.VMEM((3, blocks, LANES), F32),
            pltpu.VMEM((blocks, LANES), F32),
        ]
        + [pltpu.VMEM((blocks * frames, LANES), F32)] * 3,
        hbm_outs=() if last else (1, 2),
        cost_estimate=cost(100 * frames * features, 20 * frames * features),
        name="recur",
    )(place, gate, z if last else in_hbm(z), stats, params, valid, *arrays_of(parts))


def back_body(n_parts, spots, n_state, layer, place_ref, gate_ref, z_ref, stats_ref, params_ref, *refs):
    parts, refs = refs[:n_parts], refs[n_parts:]
    states, refs = refs[:n_state], refs[n_state:]
    slopes, refs = refs[:n_state], refs[n_state:]
    grad_ref, sums_ref, rows, spread, up_s, state_s, slope_s = refs
    frames = z_ref.shape[0]
    blocks = z_ref.shape[1] // LANES
    tall = frames + 8
    _, mean, inv_std = norm_terms(stats_ref)
    to_relative(place_ref, spread, rows, mean, 0)
    to_relative(place_ref, spread, rows, inv_std, 1)
    for row in range(blocks):
        lanes = slice(row * LANES, (row + 1) * LANES)
        base = row * frames
        up = None
        for (top, column), part in zip(spots, parts):
            if column <= row * LANES < column + part.shape[1] and part.shape[0] == frames:
                value = part[:, row * LANES - column : (row + 1) * LANES - column]
                up = value if up is None else up + value
        up_s[base : base + frames, :] = up
        state_s[row * tall : row * tall + 8, :] = jnp.zeros((8, LANES), F32)
        first = 0
        for state, slope in zip(states, slopes):
            some = state.shape[0]
            at = row * tall + 8 + first
            state_s[at : at + some, :] = state[:, lanes]
            slope_s[base + first : base + first + some, :] = slope[:, lanes]
            first += some
    decay = params_ref[3 * layer + 2]

    def step(i, carry):
        t = frames - 1 - i
        at = pl.ds(t, blocks, stride=frames)
        slope = slope_s[at, :]
        gate = gate_ref[t]
        total = gate * up_s[at, :] + carry
        up_s[at, :] = total * slope
        return total * (slope * decay + (1.0 - gate))

    lax.fori_loop(0, frames, step, jnp.zeros((blocks, LANES), F32), unroll=8)
    per = blocks // 4
    for row in range(blocks):
        lanes = slice(row * LANES, (row + 1) * LANES)
        base = row * frames
        grad = up_s[base : base + frames, :]
        grad_ref[:, lanes] = grad
        zhat = (z_ref[:, lanes] - rows[0, row : row + 1, :]) * rows[1, row : row + 1, :]
        before = state_s[row * tall + 7 : row * tall + 7 + frames, :]
        at = place_ref[row // per] * per + row % per
        for slot, value in enumerate((grad * zhat, grad, grad * before)):
            sums_ref[slot, pl.ds(at, 1), :] = jnp.sum(value, axis=0, keepdims=True)


def spots_of_sum(parts, width):
    spots, column = [], 0
    for array, _ in parts:
        spots.append((0, column % (4 * width)))
        column += array.shape[1]
    return spots


def back(layer, place, gate, z, stats, params, ups, states, slopes):
    frames, features = z.shape
    width = features // 4
    blocks = features // LANES
    whole = lambda array: pl.BlockSpec(array.shape, lambda i: (0,) * array.ndim)
    out_shape = [
        jax.ShapeDtypeStruct((frames, features), F32),
        jax.ShapeDtypeStruct((3, blocks, LANES), F32),
    ]
    if layer < LAYERS - 1:
        z, states, slopes = in_hbm(z), [in_hbm(a) for a in states], [in_hbm(a) for a in slopes]
    return call(
        partial(back_body, len(ups), spots_of_sum(ups, width), len(states), layer),
        grid=(1,),
        in_specs=[SMEM_SPEC] * 2
        + [whole(a) for a in (z, stats, params)]
        + [part_spec(up, frames) for up in ups]
        + [whole(a) for a in (*states, *slopes)],
        out_specs=[whole(a) for a in out_shape],
        out_shape=out_shape,
        scratch_shapes=[
            pltpu.VMEM((2, blocks, LANES), F32),
            pltpu.VMEM((blocks, LANES), F32),
            pltpu.VMEM((blocks * frames, LANES), F32),
            pltpu.VMEM((blocks * (frames + 8), LANES), F32),
            pltpu.VMEM((blocks * frames, LANES), F32),
        ],
        cost_estimate=cost(30 * frames * features, 20 * frames * features),
        name="back",
    )(place, gate, z, stats, params, *arrays_of(ups), *states, *slopes)


def input_terms(high_s, low_s, weights):
    width = high_s.shape[2]
    left, right = [], []
    for block, weight in enumerate(weights):
        w_high, w_low = split(weight[...].reshape(width, 2 * width))
        left += [high_s[block], low_s[block], high_s[block]]
        right += [w_high, w_high, w_low]
    return dot(jnp.concatenate(left, axis=1), jnp.concatenate(right, axis=0), NN)


def norm_back_body(split_terms, layer, cols_ref, place_ref, grad_ref, z_ref, params_ref, valid_ref, stats_ref, sums_ref, *refs):
    del cols_ref
    weights, refs = refs[:4], refs[4:]
    if split_terms:
        out_ref, leave_ref, near_term_ref, far_term_ref, sums_out_ref, *refs = refs
        term_refs, starts = (far_term_ref, near_term_ref), (0, 0)
    else:
        out_ref, leave_ref, term_ref, sums_out_ref, *refs = refs
        term_refs, starts = (term_ref, term_ref), (2 * grad_ref.shape[1] // 4, 0)
    rows, spread, high_s, low_s = refs
    blocks = z_ref.shape[1] // LANES
    width = high_s.shape[2]
    per = width // LANES

    @pl.when(pl.program_id(0) == 0)
    def _():
        count, mean, inv_std = norm_terms(stats_ref)
        to_relative(place_ref, spread, rows, mean, 0)
        to_relative(place_ref, spread, rows, inv_std, 1)
        rows[2] = rows[1] * params_ref[3 * layer]
        sums = tree([sums_ref[i : i + 3] for i in range(0, sums_ref.shape[0], 3)])
        sums_out_ref[...] = sums
        to_relative(place_ref, spread, rows, sums[0] / count, 3)
        to_relative(place_ref, spread, rows, sums[1] / count, 4)
        valid = valid_ref[...]
        for row in range(blocks):
            lanes = slice(row * LANES, (row + 1) * LANES)
            one = lambda slot: rows[slot, row : row + 1, :]
            zhat = (z_ref[:, lanes] - one(0)) * one(1)
            value = one(2) * (grad_ref[:, lanes] - valid * (one(4) + zhat * one(3)))
            out_ref[:, lanes] = value
            if (row // per) % 2:
                at = (row // per // 2) * width + (row % per) * LANES
                leave_ref[:, at : at + LANES] = value
            high, low = split(value)
            inner = slice((row % per) * LANES, (row % per + 1) * LANES)
            high_s[row // per, :, inner] = high
            low_s[row // per, :, inner] = low

    value = input_terms(high_s, low_s, weights)
    for step, (term_ref, first) in enumerate(zip(term_refs, starts)):

        @pl.when(pl.program_id(0) == step)
        def _():
            for pair in range(2):
                at = pl.multiple_of(((place_ref[0] & 1) ^ pair) * width, width)
                term_ref[:, pl.ds(first + at, width)] = value[
                    :, pair * width : (pair + 1) * width
                ]


def norm_back(columns, place, grad, z, params, valid, stats, sums, weights, layer, split_terms):
    frames, features = z.shape
    width = features // 4
    blocks = features // LANES
    whole = lambda array: pl.BlockSpec(array.shape, lambda s, cols, place: (0,) * array.ndim)
    operands = [grad, z if layer == LAYERS - 1 else in_hbm(z), params, valid, stats, sums]
    full = jax.ShapeDtypeStruct((frames, features), F32)
    half = jax.ShapeDtypeStruct((frames, 2 * width), F32)
    terms = [half, half] if split_terms else [full]
    out_shape = [full, half, *terms, jax.ShapeDtypeStruct((3, blocks, LANES), F32)]
    return call(
        partial(norm_back_body, split_terms, layer),
        grid_spec=pltpu.PrefetchScalarGridSpec(
            num_scalar_prefetch=2,
            grid=(2,),
            in_specs=[whole(a) for a in operands] + weight_specs(weights, layer),
            out_specs=[whole(a) for a in out_shape],
            scratch_shapes=[
                pltpu.VMEM((5, blocks, LANES), F32),
                pltpu.VMEM((blocks, LANES), F32),
                pltpu.VMEM((4, frames, width), BF16),
                pltpu.VMEM((4, frames, width), BF16),
            ],
        ),
        out_shape=out_shape,
        cost_estimate=cost(6 * frames * features * features, 4 * features * features),
        name="norm_back",
    )(columns, place, *operands, *[in_hbm(w) for w in weights])


def own_terms_body(n_ups, spots, cols_ref, place_ref, grad_ref, *refs):
    del cols_ref
    ups, refs = refs[:n_ups], refs[n_ups:]
    weights, refs = refs[:4], refs[4:]
    out_ref, high_s, low_s = refs
    width = high_s.shape[2]
    step = pl.program_id(0)

    @pl.when(step == 0)
    def _():
        for block in range(4):
            high, low = split(grad_ref[:, block * width : (block + 1) * width])
            high_s[block] = high
            low_s[block] = low

    value = input_terms(high_s, low_s, weights)
    for pair in range(2):
        at = pl.multiple_of(((place_ref[0] & 1) ^ pair) * width, width)
        out_ref[:, pl.ds(at, width)] = value[:, pair * width : (pair + 1) * width]
    for half in range(2):

        @pl.when(step == half)
        def _():
            first = 2 * half * width
            for (_, column), up in zip(spots, ups):
                low = max(column, first)
                high = min(column + up.shape[1], first + 2 * width)
                if low < high:
                    out_ref[:, low - first : high - first] += up[:, low - column : high - column]


def own_terms(columns, place, grad, ups, weights, layer):
    frames, features = grad.shape
    width = features // 4
    whole = lambda array: pl.BlockSpec(array.shape, lambda s, cols, place: (0,) * array.ndim)
    step_block = pl.BlockSpec((frames, 2 * width), lambda s, cols, place: (0, s))
    return call(
        partial(own_terms_body, len(ups), spots_of_sum(ups, width)),
        grid_spec=pltpu.PrefetchScalarGridSpec(
            num_scalar_prefetch=2,
            grid=(2,),
            in_specs=[whole(grad)]
            + [part_spec(up, frames) for up in ups]
            + weight_specs(weights, layer),
            out_specs=step_block,
            scratch_shapes=[pltpu.VMEM((4, frames, width), BF16)] * 2,
        ),
        out_shape=jax.ShapeDtypeStruct((frames, features), F32),
        cost_estimate=cost(6 * frames * features * features, 4 * features * features),
        name="own_terms",
    )(columns, place, grad, *arrays_of(ups), *[in_hbm(w) for w in weights])


def prepare_body(n_chunks, lists_ref, *refs):
    del lists_ref
    groups = []
    for _ in range(4):
        groups.append(refs[:n_chunks])
        refs = refs[n_chunks:]
    high_ref, low_ref = refs
    padded = high_ref.shape[0] // 2
    for side in range(2):

        @pl.when(pl.program_id(0) // 4 == side)
        def _():
            for clip in range(2):
                row = clip * padded
                for part in groups[2 * clip + side]:
                    rows = part.shape[0]
                    high, low = split(part[...])
                    high_ref[row : row + rows, :] = high
                    low_ref[row : row + rows, :] = low
                    row += rows
                rest = (clip + 1) * padded - row
                zeros = jnp.zeros((rest, high_ref.shape[1]), BF16)
                high_ref[row : row + rest, :] = zeros
                low_ref[row : row + rest, :] = zeros


def prepare(lists, groups):
    width = groups[0][0].shape[1] // 4
    frames = sum(part.shape[0] for part in groups[0])
    padded = -(-frames // LANES) * LANES
    in_specs = []
    for i, group in enumerate(groups):
        for part in group:
            if i % 2 == 0:
                index = lambda s, cols, flip=i // 2: (0, jnp.minimum(s, 3) ^ flip)
            else:
                index = lambda s, cols, flip=i // 2: (0, jnp.maximum(s - 4, 0) ^ flip)
            in_specs.append(pl.BlockSpec((part.shape[0], width), index))
    out = jax.ShapeDtypeStruct((2 * padded, 8 * width), BF16)
    return call(
        partial(prepare_body, len(groups[0])),
        grid_spec=pltpu.PrefetchScalarGridSpec(
            num_scalar_prefetch=1,
            grid=(8,),
            in_specs=in_specs,
            out_specs=[pl.BlockSpec((2 * padded, width), lambda s, cols: (0, cols[s]))] * 2,
        ),
        out_shape=[out, out],
        hbm_outs=(0, 1),
        cost_estimate=cost(0, 16 * frames * 8 * width),
        name="prepare",
    )(lists, *[in_hbm(part) for group in groups for part in group])


def product(g_high, g_low, x_high, x_low):
    return dot(g_high, x_high, NN) + (dot(g_high, x_low, NN) + dot(g_low, x_high, NN))


def weight_body(turn, place_ref, *refs):
    if turn:
        grad_ref, near_ref, x_high, x_low, kept, sent, g_high, g_low, t_high, t_low = refs

        @pl.when(pl.program_id(0) == 0)
        def _():
            frames, features = grad_ref.shape
            width = features // 4
            rows = width // 4
            padded = t_high.shape[1] // 2
            t_high[...] = jnp.zeros_like(t_high)
            t_low[...] = jnp.zeros_like(t_low)
            for clip in range(2):
                for dh in range(2):
                    if clip == 0:
                        part = grad_ref[:, 2 * dh * width : (2 * dh + 1) * width]
                    else:
                        part = near_ref[:, dh * width : (dh + 1) * width]
                    high, low = split(part.T)
                    at = (
                        slice(dh * width, (dh + 1) * width),
                        slice(clip * padded, clip * padded + frames),
                    )
                    t_high[at] = high
                    t_low[at] = low
            for group in range(8):
                first, second, dh = group // 4, group // 2 % 2, group % 2
                core = place_ref[6]
                y = place_ref[4] ^ (first * core + second * (1 - core))
                x = place_ref[5] ^ (first * (1 - core) + second * core)
                at = pl.multiple_of(dh * width + (2 * y + x) * rows, rows)
                g_high[group * rows : (group + 1) * rows, :] = t_high[pl.ds(at, rows), :]
                g_low[group * rows : (group + 1) * rows, :] = t_low[pl.ds(at, rows), :]

    else:
        g_high, g_low, x_high, x_low, kept, sent = refs
    half = g_high.shape[0] // 2
    value = product(g_high[...], g_low[...], x_high[...], x_low[...])
    kept[...] = value[:half].reshape(kept.shape)
    sent[...] = value[half:].reshape(sent.shape)


def weight_rows(half, place, grads, x_split, width):
    turn = half == 0
    whole = lambda array: pl.BlockSpec(array.shape, lambda s, place: (0,) * array.ndim)
    x_spec = pl.BlockSpec((x_split[0].shape[0], width), lambda s, place: (0, 4 * half + s))
    shape = (2, 2, width // 4, 4 * width)
    out_shape = [jax.ShapeDtypeStruct(shape, F32)] * 2
    out_specs = [pl.BlockSpec(shape[:3] + (width,), lambda s, place: (0, 0, 0, s))] * 2
    scratch = []
    if turn:
        turned = (2 * width, x_split[0].shape[0])
        out_shape += [jax.ShapeDtypeStruct(turned, BF16)] * 2
        out_specs += [whole(out_shape[-1])] * 2
        scratch = [pltpu.VMEM(turned, BF16)] * 2
    return call(
        partial(weight_body, turn),
        grid_spec=pltpu.PrefetchScalarGridSpec(
            num_scalar_prefetch=1,
            grid=(4,),
            in_specs=[whole(a) for a in grads] + [x_spec] * 2,
            out_specs=out_specs,
            scratch_shapes=scratch,
        ),
        out_shape=out_shape,
        cost_estimate=cost(12 * x_split[0].shape[0] * width * 4 * width, 4 * 8 * width * width),
        name="weight_rows",
    )(place, *grads, *[in_hbm(x) for x in x_split])


def step_body(n, *refs):
    outs = refs[2 * n :]
    column = 0
    for i in range(n):
        total = refs[2 * i][...] + refs[2 * i + 1][...]
        some = slice(column, column + total.shape[-1])
        if len(outs) == 1:
            outs[0][..., some] = total
        else:
            for j, out in enumerate(outs):
                out[..., some] = total[j]
        column += total.shape[-1]


def step_of(*pairs, cut=True):
    shape = list(pairs[0][0].shape)
    shape[-1] = sum(pair[0].shape[-1] for pair in pairs)
    out = jax.ShapeDtypeStruct(tuple(shape[1:] if cut else shape), F32)
    outs = [out, out] if cut else [out]
    whole = lambda array: pl.BlockSpec(array.shape, lambda i: (0,) * array.ndim)
    operands = [array for pair in pairs for array in pair]
    return call(
        partial(step_body, len(pairs)),
        grid=(1,),
        in_specs=[whole(a) for a in operands],
        out_specs=[whole(a) for a in outs],
        out_shape=outs,
        cost_estimate=cost(0, 4 * sum(a.size for a in operands)),
        name="reduction_step",
    )(*operands)


def plane_swap(array, step):
    pairs = []
    for i in range(8):
        over_x = (i % 2 == 0) == (step == 0)
        pairs.append((i, i ^ 2 if over_x else i ^ 4))
    return lax.ppermute(array, ("y", "x", "c"), pairs)


def plane_gather(share, *before):
    first = plane_swap(share, 0)
    second = plane_swap(share, 1)
    return [share, second, first, plane_swap(after(first, *before), 1)]


def assemble_body(groups, by_core, place_ref, *refs):
    out_ref = refs[-1]
    core = place_ref[6] if by_core else 0
    column = 0
    for group in range(groups):
        rows, columns = refs[4 * group].shape
        for i in range(4):
            first, second = i // 2, i % 2
            if by_core:
                first, second = (
                    first * core + second * (1 - core),
                    first * (1 - core) + second * core,
                )
            at = pl.multiple_of((2 * (place_ref[4] ^ first) + (place_ref[5] ^ second)) * rows, rows)
            out_ref[..., pl.ds(at, rows), column : column + columns] = refs[4 * group + i][
                ...
            ].reshape(out_ref.shape[:-2] + (rows, columns))
        column += columns


def assemble(place, groups, layer=None, onto=None, by_core=True):
    pieces = [piece for group in groups for piece in group]
    rows = pieces[0].shape[0]
    shape = (4 * rows, sum(group[0].shape[1] for group in groups))
    out_spec = pl.BlockSpec(shape, lambda i: (0, 0))
    aliases, extra, extra_specs = {}, [], []
    if layer is not None:
        out_spec = pl.BlockSpec((1, *shape), lambda i: (layer, 0, 0))
        shape = (LAYERS, *shape)
    if onto is not None:
        aliases, extra = {1 + len(pieces): 0}, [onto]
        extra_specs = [pl.BlockSpec(memory_space=pl.ANY)]
    (out,) = call(
        partial(assemble_body, len(groups), by_core),
        grid=(1,),
        out_shape=[jax.ShapeDtypeStruct(shape, F32)],
        hbm_outs=(0,),
        in_specs=[SMEM_SPEC]
        + [pl.BlockSpec(p.shape, lambda i: (0, 0)) for p in pieces]
        + extra_specs,
        out_specs=[out_spec],
        input_output_aliases=aliases,
        cost_estimate=cost(0, 8 * shape[-1] * shape[-2]),
        name="assemble",
    )(place, *pieces, *extra)
    return out


def half_features(inputs, weights, gains, shifts, decays, biases, lengths, frame_mask, grad_out):
    width, slots = inputs.shape
    clips, frames = frame_mask.shape
    depth = weights.shape[2]
    blocks = 4 * width // LANES
    y, x, h, l, c = (lax.axis_index(name) for name in ("y", "x", "h", "l", "c"))
    b = 2 * y + x
    numbers = [2 * (h ^ (rel // 2)) + (c ^ (rel % 2)) for rel in range(4)] + [y, x, c]
    place = jnp.stack(numbers).astype(jnp.int32)
    own_blocks, other_blocks = (
        jnp.stack(
            [2 * (2 * (h ^ (rel // 2)) + half) + (c ^ (rel % 2)) for rel in range(4)]
        ).astype(jnp.int32)
        for half in (l, 1 - l)
    )
    all_blocks = jnp.concatenate([own_blocks, other_blocks])
    own_columns = jnp.stack([2 * h + l, 2 * (1 - h) + l]).astype(jnp.int32)
    other_columns = jnp.stack([2 * (1 - h) + 1 - l, 2 * h + 1 - l]).astype(jnp.int32)
    rows = width // 4

    clip = 2 * h + c
    seen = lax.dynamic_index_in_dim(frame_mask, clip, 0, keepdims=False)
    length = lax.dynamic_index_in_dim(lengths, clip, 0, keepdims=False)
    moments = jnp.arange(frames, dtype=jnp.int32)
    gate = ((moments < length) & ((seen == 1) | (moments == 0))).astype(F32)
    valid = jnp.broadcast_to(gate[:, None], (frames, LANES))

    def far_share(layer):
        return lax.dynamic_slice(weights, (layer, b * rows, 0), (1, rows, depth))[0]

    def over_h(array):
        return lax.ppermute(array, "h", FLIP2)

    def over_c(array):
        return lax.ppermute(array, "c", FLIP2)

    def over_second(array):
        return plane_swap(array, 1)

    def four_of(near_rows, far_rows):
        return [
            (near_rows, 0),
            (over_c(near_rows), 1),
            (far_rows, 0),
            (over_c(far_rows), 1),
        ]

    def far_blocks(share):
        both = lax.ppermute(share, ("y", "x"), DIAGONAL)
        shares = [share, lax.ppermute(share, "x", FLIP2), lax.ppermute(share, "y", FLIP2), both]
        other = [over_c(piece) for piece in shares]
        return [assemble(place, [pieces], by_core=False) for pieces in (shares, other)]

    near = over_c(weights)
    share = far_share(0)
    close, away = pack(place, after(inputs, share), frames)
    share = over_h(share)
    away = over_h(away)
    other_close = swap_half(close)
    up_close, up_away = pack(place, after(grad_out, close), frames, waits=True)
    share = after(share, up_close, valid)
    own = four_of(close, away)
    other_away = swap_half(away)
    half_weights = [[weights, near, *far_blocks(share)]]
    params = jnp.stack([gains, shifts + biases, decays], axis=1)
    own_params = params.reshape(LAYERS * 3 * width // LANES, LANES)
    params = None

    saved = []
    for layer in range(LAYERS):
        last = layer == LAYERS - 1
        flat = layer == 0
        if layer > 0:
            others = [(swap_half(array), None) for array, _ in own]
        z, *own_flat = project(
            own_blocks, place, frames, own, half_weights[layer], layer, flat=flat
        )
        if flat:
            others = four_of(other_close, after(other_away, z))
        z, stats, *other_flat = project(
            other_blocks,
            place,
            frames,
            others,
            half_weights[layer],
            layer,
            z,
            valid,
            own_params if flat else None,
            flat,
        )
        if last:
            upstream = four_of(up_close, after(up_away, z))
        if flat:
            stats = lax.all_gather(stats, ("h", "c"), tiled=True)
            share = over_h(after(far_share(1), stats))
            stats = lax.all_gather(stats, ("y", "x"), tiled=True)
        else:
            stats = lax.all_gather(stats, ("y", "x"), tiled=True)
            stats = lax.all_gather(stats, ("h", "c"), tiled=True)
        *following, states, slopes = recur(
            layer, place, gate, z, stats, params, valid, own, last
        )
        if flat:
            *following, states, slopes, params = *following, states, slopes
            groups = [own_flat, other_flat]
        else:
            groups = [arrays_of(own), arrays_of(others)]
        groups += [[over_c(after(p, z)) for p in group] for group in groups]
        x_split = prepare(all_blocks, after(groups, slopes)) if flat else None
        if flat:
            up_away = over_h(after(up_away, x_split[0], share))
            half_weights.append([weights, near, *far_blocks(after(share, slopes))])
        saved.append((groups, x_split, z, stats, states, slopes))
        own = [(array, None) for array in following]
    close, away = following
    away = over_h(away)
    output = four_of(close, away)

    ups = upstream
    results = [None] * LAYERS
    for layer in range(LAYERS - 1, -1, -1):
        groups, x_split, z, stats, states, slopes = saved[layer]
        weight = half_weights[layer]
        grad_pre, sums = back(
            layer, place, gate, z, stats, params, ups, [states], [slopes]
        )
        plane = lax.all_gather(sums, ("y", "x"), tiled=True)
        if layer == 0:
            later, go = step_of(*[(k, after(g, plane)) for k, g in zip(stay, come)])
            plane = after(plane, later)
            go = over_second(go)
        sums = lax.all_gather(plane, ("h", "c"), tiled=True)
        grad_z, leaving, *terms, sums = norm_back(
            other_columns, place, grad_pre, z, params, valid, stats, sums, weight, layer,
            layer == 0,
        )
        leaving = over_c(leaving)
        if layer > 0:
            received = [swap_half(terms[0])]
            x_split = prepare(all_blocks, after(groups, grad_z, away))
        else:
            received = [None, swap_half(terms[1])]
            later, go = step_of((later, after(go, grad_z)))
            leaving = after(leaving, later)
            later = (later, over_h(go))
        *first, g_high, g_low = weight_rows(0, place, (grad_z, leaving), x_split, width)
        turned = (g_high, g_low)
        come = [plane_swap(first[1], 0)]
        if layer == 0:
            received[0] = swap_half(after(terms[0], received[1]))
        second = weight_rows(1, place, turned, x_split, width)
        come.append(plane_swap(second[1], 0))
        stay = (first[0], second[0])
        kept = own_terms(own_columns, place, after(grad_z, second[0]), ups, weight, layer)
        ups = [(kept, None)] + [(r, None) for r in received]
        results[layer] = lax.dynamic_index_in_dim(
            sums.reshape(3, 4, width), clip, axis=1, keepdims=False
        )

    away = merge(kept, 1, received[1])
    (later,) = step_of((later[0], after(later[1], away)), cut=False)
    away = over_h(away)
    later_first, later_second = plane_swap(later, 0), plane_swap(later, 1)
    total, go = step_of((stay[0], after(come[0], later_first)), (stay[1], come[1]))
    go = over_second(go)
    later = [later, later_second, later_first, plane_swap(after(later_first, total), 1)]
    close = merge(kept, 0, after(received[0], total))
    grad_in = four_of(close, away)
    total, go = step_of((total, after(go, close, grad_in[3][0])))
    go = over_h(go)
    grad_weights = assemble(place, after([later], total), 1)
    output = unpack(place, [(after(array, grad_weights), i) for array, i in output], frames)
    grad_in = unpack(place, [(after(array, output), i) for array, i in grad_in], frames)
    (share,) = step_of((total, after(go, grad_in)), cut=False)
    grad_weights = assemble(place, [plane_gather(share)], 0, grad_weights)
    sums = jnp.stack(results)
    return (
        output,
        grad_in,
        grad_weights,
        sums[:, 0],
        sums[:, 1],
        sums[:, 2],
        sums[:, 1],
    )


def gelu_slope(value):
    return (
        0.5 * (1.0 + jax.scipy.special.erf(value / ROOT_TWO))
        + value * jnp.exp(-0.5 * value * value) / ROOT_TWO_PI
    )


def recur_step(decay, state, inputs):
    drive_t, valid_t = inputs
    pre = drive_t + decay * state
    state = state + valid_t * (jax.nn.gelu(pre, approximate=False) - state)
    return (state, state)


def back_step(decay, carry, inputs):
    upstream_t, valid_t, pre_t = inputs
    total = upstream_t + carry
    grad_pre = total * valid_t * gelu_slope(pre_t)
    carry = total * (1.0 - valid_t) + grad_pre * decay
    return (carry, grad_pre)


def add_piece(weight, piece):
    return jnp.dot(weight, piece, precision=HIGH, preferred_element_type=jnp.float32)


def weight_columns(grad_pre_norm, piece):
    return jnp.einsum("jf,kf->jk", grad_pre_norm, piece, precision=HIGH)


def split_features(inputs, weights, gains, shifts, decays, biases, lengths, frame_mask, grad_out):
    width, slots = inputs.shape
    clips, frames_len = frame_mask.shape
    frames = jnp.arange(frames_len, dtype=jnp.int32)
    valid_grid = (
        (frames[None, :] < lengths[:, None]) & ((frame_mask == 1) | (frames[None, :] == 0))
    ).astype(jnp.float32)
    valid = valid_grid.reshape(-1)
    valid_row = valid[None, :]
    valid_time = jnp.broadcast_to(valid_grid.T[:, :, None], (frames_len, clips, width)).reshape(
        frames_len, clips * width
    )
    count_local = jnp.sum(valid)

    def to_time(array):
        return jnp.transpose(array.reshape(width, clips, frames_len), (2, 1, 0)).reshape(
            frames_len, clips * width
        )

    def from_time(array):
        return jnp.transpose(array.reshape(frames_len, clips, width), (2, 1, 0)).reshape(
            width, slots
        )

    layer_in = inputs
    saved = []
    for layer_no in range(LAYERS):
        weight = weights[layer_no]
        gathered = lax.all_gather(layer_in, "neuron", axis=0, tiled=True)
        pre_norm = add_piece(weight, gathered)
        first_sum, count = lax.psum((jnp.sum(valid_row * pre_norm, axis=1), count_local), "batch")
        mean = first_sum / count
        centered = pre_norm - mean[:, None]
        var = lax.psum(jnp.sum(valid_row * centered * centered, axis=1), "batch") / count
        inv_std = lax.rsqrt(var + EPS)
        zhat = (pre_norm - mean[:, None]) * inv_std[:, None]
        drive = gains[layer_no][:, None] * zhat + (shifts[layer_no] + biases[layer_no])[:, None]
        drive_time = to_time(drive)
        decay_wide = jnp.tile(decays[layer_no], clips)
        start_state = jnp.zeros((clips * width,), jnp.float32)
        _, states = lax.scan(
            partial(recur_step, decay_wide), start_state, (drive_time, valid_time), unroll=8
        )
        saved.append((gathered, zhat, inv_std, drive_time, states, count))
        layer_in = layer_in + valid_row * from_time(states)
    upstream = grad_out
    grad_parts = [None] * LAYERS
    for layer_no in range(LAYERS - 1, -1, -1):
        gathered, zhat, inv_std, drive_time, states, count = saved[layer_no]
        decay_wide = jnp.tile(decays[layer_no], clips)
        gain = gains[layer_no]
        previous = jnp.concatenate([jnp.zeros_like(states[:1]), states[:-1]], axis=0)
        pre_time = drive_time + decay_wide[None, :] * previous
        grad_state = to_time(valid_row * upstream)
        start_carry = jnp.zeros((clips * width,), jnp.float32)
        _, grad_pre_time = lax.scan(
            partial(back_step, decay_wide),
            start_carry,
            (grad_state, valid_time, pre_time),
            reverse=True,
            unroll=8,
        )
        decay_local = jnp.sum(
            jnp.sum(grad_pre_time * previous, axis=0).reshape(clips, width), axis=0
        )
        grad_pre = from_time(grad_pre_time)
        gain_local = jnp.sum(grad_pre * zhat, axis=1)
        shift_local = jnp.sum(grad_pre, axis=1)
        grad_gain, grad_shift, grad_decay = lax.psum(
            (gain_local, shift_local, decay_local), "batch"
        )
        grad_pre_norm = (gain * inv_std)[:, None] * (
            grad_pre - valid_row * (grad_shift[:, None] + zhat * grad_gain[:, None]) / count
        )
        weight_local = weight_columns(grad_pre_norm, gathered)
        input_terms = jnp.einsum("jk,jf->kf", weights[layer_no], grad_pre_norm, precision=HIGH)
        input_grad = lax.psum_scatter(input_terms, "neuron", scatter_dimension=0, tiled=True)
        grad_weight = lax.psum(weight_local, "batch")
        upstream = upstream + input_grad
        grad_parts[layer_no] = (grad_weight, grad_gain, grad_shift, grad_decay)
    grad_weights = jnp.stack([grad_parts[layer_no][0] for layer_no in range(LAYERS)])
    grad_gains = jnp.stack([grad_parts[layer_no][1] for layer_no in range(LAYERS)])
    grad_shifts = jnp.stack([grad_parts[layer_no][2] for layer_no in range(LAYERS)])
    grad_decays = jnp.stack([grad_parts[layer_no][3] for layer_no in range(LAYERS)])
    return (layer_in, upstream, grad_weights, grad_gains, grad_shifts, grad_decays, grad_shifts)


def solution(mesh):
    if (mesh.shape["batch"], mesh.shape["neuron"]) == (4, 8):
        cut = Mesh(mesh.devices.reshape(2, 2, 2, 2, 2), ("y", "x", "h", "l", "c"))
        batch, neuron, body = ("y", "x"), ("h", "l", "c"), half_features
    else:
        cut, batch, neuron, body = mesh, "batch", "neuron", split_features
    in_specs = (
        P(neuron, batch),
        P(None, neuron, None),
        P(None, neuron),
        P(None, neuron),
        P(None, neuron),
        P(None, neuron),
        P(batch),
        P(batch, None),
        P(neuron, batch),
    )
    out_specs = (
        P(neuron, batch),
        P(neuron, batch),
        P(None, neuron, None),
        P(None, neuron),
        P(None, neuron),
        P(None, neuron),
        P(None, neuron),
    )
    return jax.shard_map(
        body, mesh=cut, in_specs=in_specs, out_specs=out_specs, check_vma=False
    )
```

```python
from functools import partial
import math

import jax
import jax.numpy as jnp
from jax import lax
from jax.experimental import pallas as pl
from jax.experimental.pallas import tpu as pltpu
from jax.sharding import Mesh, PartitionSpec as P

LAYERS = 2
EPS = 1e-05
HIGH = lax.Precision.HIGHEST
ROOT_TWO = math.sqrt(2.0)
ROOT_TWO_PI = math.sqrt(2.0 * math.pi)
F32 = jnp.float32
BF16 = jnp.bfloat16
LANES = 128
VMEM_LIMIT = 24 * 1024 * 1024
SMEM_SPEC = pl.BlockSpec(memory_space=pltpu.SMEM)
VMEM_SPEC = pl.BlockSpec(memory_space=pltpu.VMEM)


FLIP2 = [(0, 1), (1, 0)]
DIAGONAL = [(0, 3), (1, 2), (2, 1), (3, 0)]


def swap_half(array):
    return lax.ppermute(array, "l", FLIP2)


def after(value, *others):
    return lax.optimization_barrier((value, others))[0]


def split(value):
    high = value.astype(BF16)
    return high, (value - high.astype(F32)).astype(BF16)


def dot(a, b, dims):
    return lax.dot_general(a, b, (dims, ((), ())), preferred_element_type=F32)


NT = ((1,), (1,))
NN = ((1,), (0,))


def in_hbm(array):
    return pltpu.with_memory_space_constraint(array, pltpu.HBM)


def call(body, out_shape, hbm_outs=(), **kwargs):
    if hbm_outs:
        out_shape = [
            pltpu.HBM(a.shape, a.dtype) if i in hbm_outs else a for i, a in enumerate(out_shape)
        ]
    return pl.pallas_call(
        body,
        out_shape=out_shape,
        compiler_params=pltpu.CompilerParams(vmem_limit_bytes=VMEM_LIMIT),
        **kwargs,
    )


def cost(flops, byte_count):
    return pl.CostEstimate(flops=int(flops) // 64, bytes_accessed=int(byte_count) // 64, transcendentals=0)


def pack_body(frames, place_ref, in_ref, near_ref, far_ref, turned):
    slots = in_ref.shape[1]
    for start in range(0, slots, LANES):
        turned[start : start + LANES, :] = in_ref[:, start : start + LANES].T
    for rel in range(4):
        first = pl.multiple_of(place_ref[rel] * frames, 8)
        out = (near_ref, far_ref)[rel // 2]
        out[(rel % 2) * frames : (rel % 2 + 1) * frames, :] = turned[pl.ds(first, frames), :]


def pack(place, array, frames, waits=False):
    width, slots = array.shape
    out = jax.ShapeDtypeStruct((2 * frames, width), F32)
    return call(
        partial(pack_body, frames),
        grid=(1,),
        out_shape=[out, out],
        in_specs=[SMEM_SPEC, pl.BlockSpec((width, slots), lambda i: (0, 0))],
        out_specs=[pl.BlockSpec(out.shape, lambda i: (0, 0))] * 2,
        scratch_shapes=[pltpu.VMEM((slots, width), F32)],
        hbm_outs=(0, 1) if waits else (),
        cost_estimate=cost(0, 8 * width * slots),
        name="pack",
    )(place, in_hbm(array))


def part_spec(part, frames):
    array, i = part
    if i is None:
        return pl.BlockSpec(array.shape, lambda *_: (0,) * array.ndim)
    return pl.BlockSpec((frames, array.shape[1]), lambda *_: (i, 0))


def arrays_of(parts):
    return [array for array, _ in parts]


def unpack_body(frames, place_ref, *refs):
    ins, out_ref, turned = refs[:4], refs[4], refs[5]
    slots = out_ref.shape[1]
    for rel in range(4):
        first = pl.multiple_of(place_ref[rel] * frames, 8)
        turned[pl.ds(first, frames), :] = ins[rel][...]
    for start in range(0, slots, LANES):
        out_ref[:, start : start + LANES] = turned[start : start + LANES, :].T


def unpack(place, parts, frames):
    width = parts[0][0].shape[1]
    slots = 4 * frames
    return call(
        partial(unpack_body, frames),
        grid=(1,),
        out_shape=jax.ShapeDtypeStruct((width, slots), F32),
        in_specs=[SMEM_SPEC] + [part_spec(part, frames) for part in parts],
        out_specs=pl.BlockSpec((width, slots), lambda i: (0, 0)),
        scratch_shapes=[pltpu.VMEM((slots, width), F32)],
        cost_estimate=cost(0, 8 * width * slots),
        name="unpack",
    )(place, *arrays_of(parts))


def merge_body(kept_ref, come_ref, out_ref):
    frames, columns = kept_ref.shape
    width = columns // 2
    for i in range(2):
        some = slice(i * width, (i + 1) * width)
        out_ref[i * frames : (i + 1) * frames, :] = kept_ref[:, some] + come_ref[:, some]


def merge(kept, half, come):
    frames, columns = come.shape
    return call(
        merge_body,
        grid=(1,),
        out_shape=jax.ShapeDtypeStruct((2 * frames, columns // 2), F32),
        in_specs=[
            pl.BlockSpec((frames, columns), lambda i: (0, half)),
            pl.BlockSpec((frames, columns), lambda i: (0, 0)),
        ],
        out_specs=pl.BlockSpec((2 * frames, columns // 2), lambda i: (0, 0)),
        cost_estimate=cost(0, 12 * frames * columns),
        name="merge",
    )(kept, come)


def spread_of(parts, width):
    spots, row, column = [], 0, 0
    for array, _ in parts:
        spots.append((row, column))
        if array.shape[1] == width:
            column += width
        else:
            row += array.shape[0]
    return spots


def project_body(n_parts, spots, with_acc, with_stats, with_params, flat, cols_ref, place_ref, *refs):
    del cols_ref
    parts, refs = refs[:n_parts], refs[n_parts:]
    weights, refs = refs[:4], refs[4:]
    if with_acc:
        acc_ref, refs = refs[0], refs[1:]
    if with_stats:
        valid_ref, refs = refs[0], refs[1:]
    if with_params:
        params_ref, refs = refs[0], refs[1:]
    out_ref, refs = refs[0], refs[1:]
    if with_stats:
        stats_ref, refs = refs[0], refs[1:]
    if flat:
        flat_ref, refs = refs[0], refs[1:]
    x_high, x_low = refs
    step = pl.program_id(0)
    width = x_high.shape[2]

    @pl.when(step == 0)
    def _():
        for (row, column), part in zip(spots, parts):
            rows, columns = part.shape
            for start in range(0, columns, width):
                rel = (column + start) // width
                high, low = split(part[:, start : start + width])
                x_high[rel, row : row + rows, :] = high
                x_low[rel, row : row + rows, :] = low
            if flat:
                flat_ref[row : row + rows, column : column + columns] = part[...]
        if with_acc:
            out_ref[...] = acc_ref[...]
        else:
            out_ref[...] = jnp.zeros_like(out_ref)

    stacked = jnp.concatenate([x_high[step], x_low[step], x_high[step]], axis=1)
    for block in range(4):
        w_high, w_low = split(weights[block][...].reshape(width, width))
        columns = slice(block * width, (block + 1) * width)
        out_ref[:, columns] += dot(stacked, jnp.concatenate([w_high, w_high, w_low], axis=1), NT)

    if with_stats:

        @pl.when(step == pl.num_programs(0) - 1)
        def _():
            valid = valid_ref[...]
            own = jnp.sum(valid, axis=0, keepdims=True)
            per = width // LANES
            for row in range(out_ref.shape[1] // LANES):
                z = out_ref[:, row * LANES : (row + 1) * LANES]
                total = jnp.sum(valid * z, axis=0, keepdims=True)
                centred = valid * (z - total / own)
                squares = jnp.sum(centred * centred, axis=0, keepdims=True)
                at = place_ref[row // per] * per + row % per
                stats_ref[0, pl.ds(at, 1), :] = total
                stats_ref[1, pl.ds(at, 1), :] = squares
                stats_ref[2, pl.ds(at, 1), :] = own
            if with_params:
                rest = params_ref.shape[0] - 8
                stats_ref[3] = params_ref[:8, :]
                stats_ref[4] = jnp.zeros_like(stats_ref[4])
                stats_ref[4, :rest, :] = params_ref[8:, :]


def weight_specs(weights, layer, pairs=2):
    specs = []
    for weight in weights:
        width = weight.shape[-2]
        if weight.ndim == 3:
            specs.append(
                pl.BlockSpec((1, width, pairs * width), lambda s, cols, *_: (layer, 0, cols[s]))
            )
        else:
            specs.append(pl.BlockSpec((width, pairs * width), lambda s, cols, *_: (0, cols[s])))
    return specs


def project(
    columns, place, frames, parts, weights, layer, acc=None, valid=None, params=None, flat=False
):
    width = weights[0].shape[-2]
    full = pl.BlockSpec(memory_space=pltpu.VMEM)
    in_specs = [part_spec(part, frames) for part in parts]
    in_specs += weight_specs(weights, layer, 1)
    operands = arrays_of(parts) + [in_hbm(w) for w in weights]
    array = jax.ShapeDtypeStruct((frames, 4 * width), F32)
    array_spec = pl.BlockSpec((frames, 4 * width), lambda s, cols, place: (0, 0))
    out_shape, out_specs = [array], [array_spec]
    if acc is not None:
        in_specs.append(full)
        operands.append(acc)
    if valid is not None:
        in_specs.append(full)
        operands.append(valid)
        stats = (3 if params is None else 5, 4 * width // LANES, LANES)
        out_shape.append(jax.ShapeDtypeStruct(stats, F32))
        out_specs.append(pl.BlockSpec(stats, lambda s, cols, place: (0, 0, 0)))
    if params is not None:
        in_specs.append(full)
        operands.append(params)
    if flat:
        out_shape.append(array)
        out_specs.append(array_spec)
    return call(
        partial(
            project_body,
            len(parts),
            spread_of(parts, width),
            acc is not None,
            valid is not None,
            params is not None,
            flat,
        ),
        grid_spec=pltpu.PrefetchScalarGridSpec(
            num_scalar_prefetch=2,
            grid=(4,),
            in_specs=in_specs,
            out_specs=out_specs,
            scratch_shapes=[pltpu.VMEM((4, frames, width), BF16)] * 2,
        ),
        out_shape=out_shape,
        hbm_outs=((1,) if valid is None else (0, 2)) if flat else (),
        cost_estimate=cost(2 * 3 * frames * 16 * width * width, 4 * 16 * width * width),
        name="project",
    )(columns, place, *operands)


def to_relative(place_ref, spread, rows_ref, value, slot):
    per = value.shape[0] // 4
    spread[...] = value
    for rel in range(4):
        first = place_ref[rel] * per
        for row in range(per):
            rows_ref[slot, rel * per + row : rel * per + row + 1, :] = spread[
                pl.ds(first + row, 1), :
            ]


def tree(values):
    while len(values) > 1:
        values = [a + b for a, b in zip(values[::2], values[1::2])]
    return values[0]


def norm_terms(stats_ref):
    step = stats_ref.shape[0] // 16
    each = [[stats_ref[i] for i in range(slot, stats_ref.shape[0], step)] for slot in range(3)]
    totals, squares, owns = each
    count = tree(owns)
    mean = tree(totals) / count
    away = [total / own - mean for total, own in zip(totals, owns)]
    spread = tree([s + n * a * a for s, n, a in zip(squares, owns, away)])
    return count, mean, lax.rsqrt(spread / count + EPS)


def recur_body(n_parts, spots, last, layer, spread_params, place_ref, gate_ref, z_ref, stats_ref, params_ref, valid_ref, *refs):
    parts, refs = refs[:n_parts], refs[n_parts:]
    outs, refs = refs[: 1 + last], refs[1 + last :]
    if spread_params:
        state_ref, slope_ref, params_out, rows, spread, drive_s, state_s, slope_s = refs
    else:
        state_ref, slope_ref, rows, spread, drive_s, state_s, slope_s = refs
    frames = z_ref.shape[0]
    blocks = z_ref.shape[1] // LANES
    per = blocks // 4
    if spread_params:
        for rel in range(4):
            first = place_ref[rel] * (stats_ref.shape[0] // 16)
            for row in range(LAYERS * 3 * per):
                params_out[row // per, rel * per + row % per : rel * per + row % per + 1, :] = (
                    stats_ref[first + 3 + row // 8, row % 8 : row % 8 + 1, :]
                )
        params = [params_out[3 * layer + i] for i in range(3)]
    else:
        params = [params_ref[3 * layer + i] for i in range(3)]
    _, mean, inv_std = norm_terms(stats_ref)
    to_relative(place_ref, spread, rows, mean, 0)
    to_relative(place_ref, spread, rows, inv_std, 1)
    rows[1] = rows[1] * params[0]
    rows[2] = params[1]
    decay = params[2]
    for row in range(blocks):
        z = z_ref[:, row * LANES : (row + 1) * LANES]
        drive_s[row * frames : (row + 1) * frames, :] = (
            z - rows[0, row : row + 1, :]
        ) * rows[1, row : row + 1, :] + rows[2, row : row + 1, :]

    def step(t, state):
        at = pl.ds(t, blocks, stride=frames)
        pre = drive_s[at, :] + decay * state
        half = 0.5 + 0.5 * lax.erf(pre * (1.0 / ROOT_TWO))
        gate = gate_ref[t] > 0.0
        slope = half + pre * jnp.exp(-0.5 * pre * pre) * (1.0 / ROOT_TWO_PI)
        state = jnp.where(gate, pre * half, state)
        state_s[at, :] = state
        slope_s[at, :] = jnp.where(gate, slope, 0.0)
        return state

    lax.fori_loop(0, frames, step, jnp.zeros((blocks, LANES), F32), unroll=8)
    valid = valid_ref[...]
    for row in range(blocks):
        lanes = slice(row * LANES, (row + 1) * LANES)
        state = state_s[row * frames : (row + 1) * frames, :]
        state_ref[:, lanes] = state
        slope_ref[:, lanes] = slope_s[row * frames : (row + 1) * frames, :]
        for (top, column), part in zip(spots, parts):
            if column <= row * LANES < column + part.shape[1]:
                x = part[:, row * LANES - column : (row + 1) * LANES - column]
                some = slice(top, top + part.shape[0])
                value = x + valid[some] * state[some]
                if last:
                    rel, at = divmod(row * LANES, outs[0].shape[1])
                    base = top + frames * (rel % 2)
                    outs[rel // 2][base : base + part.shape[0], at : at + LANES] = value
                else:
                    outs[0][top : top + part.shape[0], lanes] = value


def recur(layer, place, gate, z, stats, params, valid, parts, last):
    frames, features = z.shape
    width = features // 4
    blocks = features // LANES
    whole = lambda array: pl.BlockSpec(array.shape, lambda i: (0,) * array.ndim)
    full = jax.ShapeDtypeStruct((frames, features), F32)
    outs = [jax.ShapeDtypeStruct((2 * frames, width), F32)] * 2 if last else [full]
    out_shape = outs + [full, full]
    spread_params = params is None
    if spread_params:
        out_shape.append(jax.ShapeDtypeStruct((3 * LAYERS, blocks, LANES), F32))
        params = valid
    return call(
        partial(recur_body, len(parts), spread_of(parts, width), last, layer, spread_params),
        grid=(1,),
        in_specs=[SMEM_SPEC, SMEM_SPEC]
        + [whole(a) for a in (z, stats, params, valid)]
        + [part_spec(part, frames) for part in parts],
        out_specs=[whole(s) for s in out_shape],
        out_shape=out_shape,
        scratch_shapes=[
            pltpu.VMEM((3, blocks, LANES), F32),
            pltpu.VMEM((blocks, LANES), F32),
        ]
        + [pltpu.VMEM((blocks * frames, LANES), F32)] * 3,
        hbm_outs=() if last else (1, 2),
        cost_estimate=cost(100 * frames * features, 20 * frames * features),
        name="recur",
    )(place, gate, z if last else in_hbm(z), stats, params, valid, *arrays_of(parts))


def back_body(n_parts, spots, n_state, layer, place_ref, gate_ref, z_ref, stats_ref, params_ref, *refs):
    parts, refs = refs[:n_parts], refs[n_parts:]
    states, refs = refs[:n_state], refs[n_state:]
    slopes, refs = refs[:n_state], refs[n_state:]
    grad_ref, sums_ref, rows, spread, up_s, state_s, slope_s = refs
    frames = z_ref.shape[0]
    blocks = z_ref.shape[1] // LANES
    tall = frames + 8
    _, mean, inv_std = norm_terms(stats_ref)
    to_relative(place_ref, spread, rows, mean, 0)
    to_relative(place_ref, spread, rows, inv_std, 1)
    for row in range(blocks):
        lanes = slice(row * LANES, (row + 1) * LANES)
        base = row * frames
        up = None
        for (top, column), part in zip(spots, parts):
            if column <= row * LANES < column + part.shape[1] and part.shape[0] == frames:
                value = part[:, row * LANES - column : (row + 1) * LANES - column]
                up = value if up is None else up + value
        up_s[base : base + frames, :] = up
        state_s[row * tall : row * tall + 8, :] = jnp.zeros((8, LANES), F32)
        first = 0
        for state, slope in zip(states, slopes):
            some = state.shape[0]
            at = row * tall + 8 + first
            state_s[at : at + some, :] = state[:, lanes]
            slope_s[base + first : base + first + some, :] = slope[:, lanes]
            first += some
    decay = params_ref[3 * layer + 2]

    def step(i, carry):
        t = frames - 1 - i
        at = pl.ds(t, blocks, stride=frames)
        slope = slope_s[at, :]
        gate = gate_ref[t]
        total = gate * up_s[at, :] + carry
        up_s[at, :] = total * slope
        return total * (slope * decay + (1.0 - gate))

    lax.fori_loop(0, frames, step, jnp.zeros((blocks, LANES), F32), unroll=8)
    per = blocks // 4
    for row in range(blocks):
        lanes = slice(row * LANES, (row + 1) * LANES)
        base = row * frames
        grad = up_s[base : base + frames, :]
        grad_ref[:, lanes] = grad
        zhat = (z_ref[:, lanes] - rows[0, row : row + 1, :]) * rows[1, row : row + 1, :]
        before = state_s[row * tall + 7 : row * tall + 7 + frames, :]
        at = place_ref[row // per] * per + row % per
        for slot, value in enumerate((grad * zhat, grad, grad * before)):
            sums_ref[slot, pl.ds(at, 1), :] = jnp.sum(value, axis=0, keepdims=True)


def spots_of_sum(parts, width):
    spots, column = [], 0
    for array, _ in parts:
        spots.append((0, column % (4 * width)))
        column += array.shape[1]
    return spots


def back(layer, place, gate, z, stats, params, ups, states, slopes):
    frames, features = z.shape
    width = features // 4
    blocks = features // LANES
    whole = lambda array: pl.BlockSpec(array.shape, lambda i: (0,) * array.ndim)
    out_shape = [
        jax.ShapeDtypeStruct((frames, features), F32),
        jax.ShapeDtypeStruct((3, blocks, LANES), F32),
    ]
    if layer < LAYERS - 1:
        z, states, slopes = in_hbm(z), [in_hbm(a) for a in states], [in_hbm(a) for a in slopes]
    return call(
        partial(back_body, len(ups), spots_of_sum(ups, width), len(states), layer),
        grid=(1,),
        in_specs=[SMEM_SPEC] * 2
        + [whole(a) for a in (z, stats, params)]
        + [part_spec(up, frames) for up in ups]
        + [whole(a) for a in (*states, *slopes)],
        out_specs=[whole(a) for a in out_shape],
        out_shape=out_shape,
        scratch_shapes=[
            pltpu.VMEM((2, blocks, LANES), F32),
            pltpu.VMEM((blocks, LANES), F32),
            pltpu.VMEM((blocks * frames, LANES), F32),
            pltpu.VMEM((blocks * (frames + 8), LANES), F32),
            pltpu.VMEM((blocks * frames, LANES), F32),
        ],
        cost_estimate=cost(30 * frames * features, 20 * frames * features),
        name="back",
    )(place, gate, z, stats, params, *arrays_of(ups), *states, *slopes)


def input_terms(high_s, low_s, weights):
    width = high_s.shape[2]
    left, right = [], []
    for block, weight in enumerate(weights):
        w_high, w_low = split(weight[...].reshape(width, 2 * width))
        left += [high_s[block], low_s[block], high_s[block]]
        right += [w_high, w_high, w_low]
    return dot(jnp.concatenate(left, axis=1), jnp.concatenate(right, axis=0), NN)


def norm_back_body(split_terms, layer, cols_ref, place_ref, grad_ref, z_ref, params_ref, valid_ref, stats_ref, sums_ref, *refs):
    del cols_ref
    weights, refs = refs[:4], refs[4:]
    if split_terms:
        out_ref, leave_ref, near_term_ref, far_term_ref, sums_out_ref, *refs = refs
        term_refs, starts = (far_term_ref, near_term_ref), (0, 0)
    else:
        out_ref, leave_ref, term_ref, sums_out_ref, *refs = refs
        term_refs, starts = (term_ref, term_ref), (2 * grad_ref.shape[1] // 4, 0)
    rows, spread, high_s, low_s = refs
    blocks = z_ref.shape[1] // LANES
    width = high_s.shape[2]
    per = width // LANES

    @pl.when(pl.program_id(0) == 0)
    def _():
        count, mean, inv_std = norm_terms(stats_ref)
        to_relative(place_ref, spread, rows, mean, 0)
        to_relative(place_ref, spread, rows, inv_std, 1)
        rows[2] = rows[1] * params_ref[3 * layer]
        sums = tree([sums_ref[i : i + 3] for i in range(0, sums_ref.shape[0], 3)])
        sums_out_ref[...] = sums
        to_relative(place_ref, spread, rows, sums[0] / count, 3)
        to_relative(place_ref, spread, rows, sums[1] / count, 4)
        valid = valid_ref[...]
        for row in range(blocks):
            lanes = slice(row * LANES, (row + 1) * LANES)
            one = lambda slot: rows[slot, row : row + 1, :]
            zhat = (z_ref[:, lanes] - one(0)) * one(1)
            value = one(2) * (grad_ref[:, lanes] - valid * (one(4) + zhat * one(3)))
            out_ref[:, lanes] = value
            if (row // per) % 2:
                at = (row // per // 2) * width + (row % per) * LANES
                leave_ref[:, at : at + LANES] = value
            high, low = split(value)
            inner = slice((row % per) * LANES, (row % per + 1) * LANES)
            high_s[row // per, :, inner] = high
            low_s[row // per, :, inner] = low

    value = input_terms(high_s, low_s, weights)
    for step, (term_ref, first) in enumerate(zip(term_refs, starts)):

        @pl.when(pl.program_id(0) == step)
        def _():
            for pair in range(2):
                at = pl.multiple_of(((place_ref[0] & 1) ^ pair) * width, width)
                term_ref[:, pl.ds(first + at, width)] = value[
                    :, pair * width : (pair + 1) * width
                ]


def norm_back(columns, place, grad, z, params, valid, stats, sums, weights, layer, split_terms):
    frames, features = z.shape
    width = features // 4
    blocks = features // LANES
    whole = lambda array: pl.BlockSpec(array.shape, lambda s, cols, place: (0,) * array.ndim)
    operands = [grad, z if layer == LAYERS - 1 else in_hbm(z), params, valid, stats, sums]
    full = jax.ShapeDtypeStruct((frames, features), F32)
    half = jax.ShapeDtypeStruct((frames, 2 * width), F32)
    terms = [half, half] if split_terms else [full]
    out_shape = [full, half, *terms, jax.ShapeDtypeStruct((3, blocks, LANES), F32)]
    return call(
        partial(norm_back_body, split_terms, layer),
        grid_spec=pltpu.PrefetchScalarGridSpec(
            num_scalar_prefetch=2,
            grid=(2,),
            in_specs=[whole(a) for a in operands] + weight_specs(weights, layer),
            out_specs=[whole(a) for a in out_shape],
            scratch_shapes=[
                pltpu.VMEM((5, blocks, LANES), F32),
                pltpu.VMEM((blocks, LANES), F32),
                pltpu.VMEM((4, frames, width), BF16),
                pltpu.VMEM((4, frames, width), BF16),
            ],
        ),
        out_shape=out_shape,
        cost_estimate=cost(6 * frames * features * features, 4 * features * features),
        name="norm_back",
    )(columns, place, *operands, *[in_hbm(w) for w in weights])


def own_terms_body(n_ups, spots, cols_ref, place_ref, grad_ref, *refs):
    del cols_ref
    ups, refs = refs[:n_ups], refs[n_ups:]
    weights, refs = refs[:4], refs[4:]
    out_ref, high_s, low_s = refs
    width = high_s.shape[2]
    step = pl.program_id(0)

    @pl.when(step == 0)
    def _():
        for block in range(4):
            high, low = split(grad_ref[:, block * width : (block + 1) * width])
            high_s[block] = high
            low_s[block] = low

    value = input_terms(high_s, low_s, weights)
    for pair in range(2):
        at = pl.multiple_of(((place_ref[0] & 1) ^ pair) * width, width)
        out_ref[:, pl.ds(at, width)] = value[:, pair * width : (pair + 1) * width]
    for half in range(2):

        @pl.when(step == half)
        def _():
            first = 2 * half * width
            for (_, column), up in zip(spots, ups):
                low = max(column, first)
                high = min(column + up.shape[1], first + 2 * width)
                if low < high:
                    out_ref[:, low - first : high - first] += up[:, low - column : high - column]


def own_terms(columns, place, grad, ups, weights, layer):
    frames, features = grad.shape
    width = features // 4
    whole = lambda array: pl.BlockSpec(array.shape, lambda s, cols, place: (0,) * array.ndim)
    step_block = pl.BlockSpec((frames, 2 * width), lambda s, cols, place: (0, s))
    return call(
        partial(own_terms_body, len(ups), spots_of_sum(ups, width)),
        grid_spec=pltpu.PrefetchScalarGridSpec(
            num_scalar_prefetch=2,
            grid=(2,),
            in_specs=[whole(grad)]
            + [part_spec(up, frames) for up in ups]
            + weight_specs(weights, layer),
            out_specs=step_block,
            scratch_shapes=[pltpu.VMEM((4, frames, width), BF16)] * 2,
        ),
        out_shape=jax.ShapeDtypeStruct((frames, features), F32),
        cost_estimate=cost(6 * frames * features * features, 4 * features * features),
        name="own_terms",
    )(columns, place, grad, *arrays_of(ups), *[in_hbm(w) for w in weights])


def prepare_body(n_chunks, lists_ref, *refs):
    del lists_ref
    groups = []
    for _ in range(4):
        groups.append(refs[:n_chunks])
        refs = refs[n_chunks:]
    high_ref, low_ref = refs
    padded = high_ref.shape[0] // 2
    for side in range(2):

        @pl.when(pl.program_id(0) // 4 == side)
        def _():
            for clip in range(2):
                row = clip * padded
                for part in groups[2 * clip + side]:
                    rows = part.shape[0]
                    high, low = split(part[...])
                    high_ref[row : row + rows, :] = high
                    low_ref[row : row + rows, :] = low
                    row += rows
                rest = (clip + 1) * padded - row
                zeros = jnp.zeros((rest, high_ref.shape[1]), BF16)
                high_ref[row : row + rest, :] = zeros
                low_ref[row : row + rest, :] = zeros


def prepare(lists, groups):
    width = groups[0][0].shape[1] // 4
    frames = sum(part.shape[0] for part in groups[0])
    padded = -(-frames // LANES) * LANES
    in_specs = []
    for i, group in enumerate(groups):
        for part in group:
            if i % 2 == 0:
                index = lambda s, cols, flip=i // 2: (0, jnp.minimum(s, 3) ^ flip)
            else:
                index = lambda s, cols, flip=i // 2: (0, jnp.maximum(s - 4, 0) ^ flip)
            in_specs.append(pl.BlockSpec((part.shape[0], width), index))
    out = jax.ShapeDtypeStruct((2 * padded, 8 * width), BF16)
    return call(
        partial(prepare_body, len(groups[0])),
        grid_spec=pltpu.PrefetchScalarGridSpec(
            num_scalar_prefetch=1,
            grid=(8,),
            in_specs=in_specs,
            out_specs=[pl.BlockSpec((2 * padded, width), lambda s, cols: (0, cols[s]))] * 2,
        ),
        out_shape=[out, out],
        hbm_outs=(0, 1),
        cost_estimate=cost(0, 16 * frames * 8 * width),
        name="prepare",
    )(lists, *[in_hbm(part) for group in groups for part in group])


def product(g_high, g_low, x_high, x_low):
    return dot(g_high, x_high, NN) + (dot(g_high, x_low, NN) + dot(g_low, x_high, NN))


def weight_body(turn, place_ref, *refs):
    if turn:
        grad_ref, near_ref, x_high, x_low, kept, sent, g_high, g_low, t_high, t_low = refs

        @pl.when(pl.program_id(0) == 0)
        def _():
            frames, features = grad_ref.shape
            width = features // 4
            rows = width // 4
            padded = t_high.shape[1] // 2
            t_high[...] = jnp.zeros_like(t_high)
            t_low[...] = jnp.zeros_like(t_low)
            for clip in range(2):
                for dh in range(2):
                    if clip == 0:
                        part = grad_ref[:, 2 * dh * width : (2 * dh + 1) * width]
                    else:
                        part = near_ref[:, dh * width : (dh + 1) * width]
                    high, low = split(part.T)
                    at = (
                        slice(dh * width, (dh + 1) * width),
                        slice(clip * padded, clip * padded + frames),
                    )
                    t_high[at] = high
                    t_low[at] = low
            for group in range(8):
                first, second, dh = group // 4, group // 2 % 2, group % 2
                core = place_ref[6]
                y = place_ref[4] ^ (first * core + second * (1 - core))
                x = place_ref[5] ^ (first * (1 - core) + second * core)
                at = pl.multiple_of(dh * width + (2 * y + x) * rows, rows)
                g_high[group * rows : (group + 1) * rows, :] = t_high[pl.ds(at, rows), :]
                g_low[group * rows : (group + 1) * rows, :] = t_low[pl.ds(at, rows), :]

    else:
        g_high, g_low, x_high, x_low, kept, sent = refs
    half = g_high.shape[0] // 2
    value = product(g_high[...], g_low[...], x_high[...], x_low[...])
    kept[...] = value[:half].reshape(kept.shape)
    sent[...] = value[half:].reshape(sent.shape)


def weight_rows(half, place, grads, x_split, width):
    turn = half == 0
    whole = lambda array: pl.BlockSpec(array.shape, lambda s, place: (0,) * array.ndim)
    x_spec = pl.BlockSpec((x_split[0].shape[0], width), lambda s, place: (0, 4 * half + s))
    shape = (2, 2, width // 4, 4 * width)
    out_shape = [jax.ShapeDtypeStruct(shape, F32)] * 2
    out_specs = [pl.BlockSpec(shape[:3] + (width,), lambda s, place: (0, 0, 0, s))] * 2
    scratch = []
    if turn:
        turned = (2 * width, x_split[0].shape[0])
        out_shape += [jax.ShapeDtypeStruct(turned, BF16)] * 2
        out_specs += [whole(out_shape[-1])] * 2
        scratch = [pltpu.VMEM(turned, BF16)] * 2
    return call(
        partial(weight_body, turn),
        grid_spec=pltpu.PrefetchScalarGridSpec(
            num_scalar_prefetch=1,
            grid=(4,),
            in_specs=[whole(a) for a in grads] + [x_spec] * 2,
            out_specs=out_specs,
            scratch_shapes=scratch,
        ),
        out_shape=out_shape,
        cost_estimate=cost(12 * x_split[0].shape[0] * width * 4 * width, 4 * 8 * width * width),
        name="weight_rows",
    )(place, *grads, *[in_hbm(x) for x in x_split])


def step_body(n, cut, *refs):
    ins, outs = refs[: 2 * n], refs[2 * n :]
    columns = outs[0].shape[-1]
    column = 0
    for i in range(n):
        total = ins[2 * i][...] + ins[2 * i + 1][...]
        for first in range(0, total.shape[-1], columns):
            at = (column + first) % columns
            rest = min(columns - at, total.shape[-1] - first)
            to = (Ellipsis, slice(at, at + rest))
            piece = total[..., first : first + rest]
            out = (column + first) // columns
            if cut:
                outs[2 * out][to] = piece[0]
                outs[2 * out + 1][to] = piece[1]
            else:
                outs[out][to] = piece
        column += total.shape[-1]


def step_of(*pairs, cut=True, halves=1):
    shape = list(pairs[0][0].shape)
    shape[-1] = sum(pair[0].shape[-1] for pair in pairs) // halves
    out = jax.ShapeDtypeStruct(tuple(shape[1:] if cut else shape), F32)
    outs = [out] * (halves * (1 + cut))
    whole = lambda array: pl.BlockSpec(array.shape, lambda i: (0,) * array.ndim)
    operands = [array for pair in pairs for array in pair]
    return call(
        partial(step_body, len(pairs), cut),
        grid=(1,),
        in_specs=[whole(a) for a in operands],
        out_specs=[whole(a) for a in outs],
        out_shape=outs,
        cost_estimate=cost(0, 4 * sum(a.size for a in operands)),
        name="reduction_step",
    )(*operands)


def plane_swap(array, step):
    pairs = []
    for i in range(8):
        over_x = (i % 2 == 0) == (step == 0)
        pairs.append((i, i ^ 2 if over_x else i ^ 4))
    return lax.ppermute(array, ("y", "x", "c"), pairs)


def plane_gather(share, *before):
    first = plane_swap(share, 0)
    second = plane_swap(share, 1)
    return [share, second, first, plane_swap(after(first, *before), 1)]


def assemble_body(groups, by_core, place_ref, *refs):
    out_ref = refs[-1]
    core = place_ref[6] if by_core else 0
    column = 0
    for group in range(groups):
        rows, columns = refs[4 * group].shape
        for i in range(4):
            first, second = i // 2, i % 2
            if by_core:
                first, second = (
                    first * core + second * (1 - core),
                    first * (1 - core) + second * core,
                )
            at = pl.multiple_of((2 * (place_ref[4] ^ first) + (place_ref[5] ^ second)) * rows, rows)
            out_ref[..., pl.ds(at, rows), column : column + columns] = refs[4 * group + i][
                ...
            ].reshape(out_ref.shape[:-2] + (rows, columns))
        column += columns


def assemble(place, groups, layer=None, onto=None, by_core=True):
    pieces = [piece for group in groups for piece in group]
    rows = pieces[0].shape[0]
    shape = (4 * rows, sum(group[0].shape[1] for group in groups))
    out_spec = pl.BlockSpec(shape, lambda i: (0, 0))
    aliases, extra, extra_specs = {}, [], []
    if layer is not None:
        out_spec = pl.BlockSpec((1, *shape), lambda i: (layer, 0, 0))
        shape = (LAYERS, *shape)
    if onto is not None:
        aliases, extra = {1 + len(pieces): 0}, [onto]
        extra_specs = [pl.BlockSpec(memory_space=pl.ANY)]
    (out,) = call(
        partial(assemble_body, len(groups), by_core),
        grid=(1,),
        out_shape=[jax.ShapeDtypeStruct(shape, F32)],
        hbm_outs=(0,),
        in_specs=[SMEM_SPEC]
        + [pl.BlockSpec(p.shape, lambda i: (0, 0)) for p in pieces]
        + extra_specs,
        out_specs=[out_spec],
        input_output_aliases=aliases,
        cost_estimate=cost(0, 8 * shape[-1] * shape[-2]),
        name="assemble",
    )(place, *pieces, *extra)
    return out


def half_features(inputs, weights, gains, shifts, decays, biases, lengths, frame_mask, grad_out):
    width, slots = inputs.shape
    clips, frames = frame_mask.shape
    depth = weights.shape[2]
    blocks = 4 * width // LANES
    y, x, h, l, c = (lax.axis_index(name) for name in ("y", "x", "h", "l", "c"))
    b = 2 * y + x
    numbers = [2 * (h ^ (rel // 2)) + (c ^ (rel % 2)) for rel in range(4)] + [y, x, c]
    place = jnp.stack(numbers).astype(jnp.int32)
    own_blocks, other_blocks = (
        jnp.stack(
            [2 * (2 * (h ^ (rel // 2)) + half) + (c ^ (rel % 2)) for rel in range(4)]
        ).astype(jnp.int32)
        for half in (l, 1 - l)
    )
    all_blocks = jnp.concatenate([own_blocks, other_blocks])
    own_columns = jnp.stack([2 * h + l, 2 * (1 - h) + l]).astype(jnp.int32)
    other_columns = jnp.stack([2 * (1 - h) + 1 - l, 2 * h + 1 - l]).astype(jnp.int32)
    rows = width // 4

    clip = 2 * h + c
    seen = lax.dynamic_index_in_dim(frame_mask, clip, 0, keepdims=False)
    length = lax.dynamic_index_in_dim(lengths, clip, 0, keepdims=False)
    moments = jnp.arange(frames, dtype=jnp.int32)
    gate = ((moments < length) & ((seen == 1) | (moments == 0))).astype(F32)
    valid = jnp.broadcast_to(gate[:, None], (frames, LANES))

    def far_share(layer):
        return lax.dynamic_slice(weights, (layer, b * rows, 0), (1, rows, depth))[0]

    def over_h(array):
        return lax.ppermute(array, "h", FLIP2)

    def over_c(array):
        return lax.ppermute(array, "c", FLIP2)

    def over_second(array):
        return plane_swap(array, 1)

    def four_of(near_rows, far_rows):
        return [
            (near_rows, 0),
            (over_c(near_rows), 1),
            (far_rows, 0),
            (over_c(far_rows), 1),
        ]

    def far_blocks(share):
        both = lax.ppermute(share, ("y", "x"), DIAGONAL)
        shares = [share, lax.ppermute(share, "x", FLIP2), lax.ppermute(share, "y", FLIP2), both]
        other = [over_c(piece) for piece in shares]
        return [assemble(place, [pieces], by_core=False) for pieces in (shares, other)]

    near = over_c(weights)
    share = far_share(0)
    close, away = pack(place, after(inputs, share), frames)
    share = over_h(share)
    away = over_h(away)
    other_close = swap_half(close)
    up_close, up_away = pack(place, after(grad_out, close), frames, waits=True)
    share = after(share, up_close, valid)
    own = four_of(close, away)
    other_away = swap_half(away)
    half_weights = [[weights, near, *far_blocks(share)]]
    share = over_h(after(far_share(1), away))
    params = jnp.stack([gains, shifts + biases, decays], axis=1)
    own_params = params.reshape(LAYERS * 3 * width // LANES, LANES)
    params = None

    saved = []
    for layer in range(LAYERS):
        last = layer == LAYERS - 1
        flat = layer == 0
        if layer > 0:
            others = [(swap_half(array), None) for array, _ in own]
        z, *own_flat = project(
            own_blocks, place, frames, own, half_weights[layer], layer, flat=flat
        )
        if flat:
            others = four_of(other_close, after(other_away, z, share))
        z, stats, *other_flat = project(
            other_blocks,
            place,
            frames,
            others,
            half_weights[layer],
            layer,
            z,
            valid,
            own_params if flat else None,
            flat,
        )
        if last:
            upstream = four_of(up_close, after(up_away, z))
        if flat:
            stats = lax.all_gather(stats, ("h", "c"), tiled=True)
            stats = lax.all_gather(stats, ("y", "x"), tiled=True)
        else:
            stats = lax.all_gather(stats, ("y", "x"), tiled=True)
            stats = lax.all_gather(stats, ("h", "c"), tiled=True)
        *following, states, slopes = recur(
            layer, place, gate, z, stats, params, valid, own, last
        )
        if flat:
            *following, states, slopes, params = *following, states, slopes
            groups = [own_flat, other_flat]
        else:
            groups = [arrays_of(own), arrays_of(others)]
        groups += [[over_c(after(p, z)) for p in group] for group in groups]
        x_split = prepare(all_blocks, after(groups, slopes)) if flat else None
        if flat:
            up_away = over_h(after(up_away, x_split[0]))
            half_weights.append([weights, near, *far_blocks(after(share, slopes))])
        saved.append((groups, x_split, z, stats, states, slopes))
        own = [(array, None) for array in following]
    output_close, output_away = following
    output_away = over_h(output_away)
    output = four_of(output_close, output_away)

    ups = upstream
    results = [None] * LAYERS
    for layer in range(LAYERS - 1, -1, -1):
        groups, x_split, z, stats, states, slopes = saved[layer]
        weight = half_weights[layer]
        grad_pre, sums = back(
            layer, place, gate, z, stats, params, ups, [states], [slopes]
        )
        plane = lax.all_gather(sums, ("y", "x"), tiled=True)
        if layer == 0:
            later, go = step_of(*[(k, after(g, plane)) for k, g in zip(stay, come)])
            plane = after(plane, later)
            go = over_second(go)
        sums = lax.all_gather(plane, ("h", "c"), tiled=True)
        grad_z, leaving, *terms, sums = norm_back(
            other_columns, place, grad_pre, z, params, valid, stats, sums, weight, layer,
            layer == 0,
        )
        leaving = over_c(leaving)
        if layer > 0:
            received = [swap_half(terms[0])]
            x_split = prepare(all_blocks, after(groups, grad_z, output_away))
        else:
            received = [None, swap_half(terms[1])]
            later, go = step_of((later, after(go, grad_z)))
            leaving = after(leaving, later)
            later = (later, over_h(go))
        *first, g_high, g_low = weight_rows(0, place, (grad_z, leaving), x_split, width)
        turned = (g_high, g_low)
        come = [plane_swap(first[1], 0)]
        if layer == 0:
            received[0] = swap_half(after(terms[0], received[1]))
        second = weight_rows(1, place, turned, x_split, width)
        come.append(plane_swap(second[1], 0))
        stay = (first[0], second[0])
        kept = own_terms(own_columns, place, after(grad_z, second[0]), ups, weight, layer)
        ups = [(kept, None)] + [(r, None) for r in received]
        results[layer] = lax.dynamic_index_in_dim(
            sums.reshape(3, 4, width), clip, axis=1, keepdims=False
        )

    away = merge(kept, 1, received[1])
    (later,) = step_of((later[0], after(later[1], away)), cut=False)
    away = over_h(away)
    later_first, later_second = plane_swap(later, 0), plane_swap(later, 1)
    total, go = step_of((stay[0], after(come[0], later_first)), (stay[1], come[1]))
    go = over_second(go)
    later = [later, later_second, later_first, plane_swap(after(later_first, total), 1)]
    far = [(away, 0), (over_c(away), 1)]
    stay0, go0, stay1, go1 = step_of((total, after(go, far[1][0])), halves=2)
    go0, go1 = over_h(go0), over_h(go1)
    grad_weights = assemble(place, after([later], stay0), 1)
    output = unpack(place, [(after(array, grad_weights), i) for array, i in output], frames)
    (share,) = step_of((stay0, after(go0, output)), cut=False)
    gathered = [plane_gather(share)]
    close = merge(kept, 0, after(received[0], share))
    close = [(close, 0), (over_c(close), 1)]
    (share,) = step_of((stay1, after(go1, close[0][0])), cut=False)
    gathered.append(plane_gather(share))
    grad_in = unpack(place, [(after(array, share), i) for array, i in close + far], frames)
    grad_weights = assemble(place, after(gathered, grad_in), 0, grad_weights)
    sums = jnp.stack(results)
    return (
        output,
        grad_in,
        grad_weights,
        sums[:, 0],
        sums[:, 1],
        sums[:, 2],
        sums[:, 1],
    )


def gelu_slope(value):
    return (
        0.5 * (1.0 + jax.scipy.special.erf(value / ROOT_TWO))
        + value * jnp.exp(-0.5 * value * value) / ROOT_TWO_PI
    )


def recur_step(decay, state, inputs):
    drive_t, valid_t = inputs
    pre = drive_t + decay * state
    state = state + valid_t * (jax.nn.gelu(pre, approximate=False) - state)
    return (state, state)


def back_step(decay, carry, inputs):
    upstream_t, valid_t, pre_t = inputs
    total = upstream_t + carry
    grad_pre = total * valid_t * gelu_slope(pre_t)
    carry = total * (1.0 - valid_t) + grad_pre * decay
    return (carry, grad_pre)


def add_piece(weight, piece):
    return jnp.dot(weight, piece, precision=HIGH, preferred_element_type=jnp.float32)


def weight_columns(grad_pre_norm, piece):
    return jnp.einsum("jf,kf->jk", grad_pre_norm, piece, precision=HIGH)


def split_features(inputs, weights, gains, shifts, decays, biases, lengths, frame_mask, grad_out):
    width, slots = inputs.shape
    clips, frames_len = frame_mask.shape
    frames = jnp.arange(frames_len, dtype=jnp.int32)
    valid_grid = (
        (frames[None, :] < lengths[:, None]) & ((frame_mask == 1) | (frames[None, :] == 0))
    ).astype(jnp.float32)
    valid = valid_grid.reshape(-1)
    valid_row = valid[None, :]
    valid_time = jnp.broadcast_to(valid_grid.T[:, :, None], (frames_len, clips, width)).reshape(
        frames_len, clips * width
    )
    count_local = jnp.sum(valid)

    def to_time(array):
        return jnp.transpose(array.reshape(width, clips, frames_len), (2, 1, 0)).reshape(
            frames_len, clips * width
        )

    def from_time(array):
        return jnp.transpose(array.reshape(frames_len, clips, width), (2, 1, 0)).reshape(
            width, slots
        )

    layer_in = inputs
    saved = []
    for layer_no in range(LAYERS):
        weight = weights[layer_no]
        gathered = lax.all_gather(layer_in, "neuron", axis=0, tiled=True)
        pre_norm = add_piece(weight, gathered)
        first_sum, count = lax.psum((jnp.sum(valid_row * pre_norm, axis=1), count_local), "batch")
        mean = first_sum / count
        centered = pre_norm - mean[:, None]
        var = lax.psum(jnp.sum(valid_row * centered * centered, axis=1), "batch") / count
        inv_std = lax.rsqrt(var + EPS)
        zhat = (pre_norm - mean[:, None]) * inv_std[:, None]
        drive = gains[layer_no][:, None] * zhat + (shifts[layer_no] + biases[layer_no])[:, None]
        drive_time = to_time(drive)
        decay_wide = jnp.tile(decays[layer_no], clips)
        start_state = jnp.zeros((clips * width,), jnp.float32)
        _, states = lax.scan(
            partial(recur_step, decay_wide), start_state, (drive_time, valid_time), unroll=8
        )
        saved.append((gathered, zhat, inv_std, drive_time, states, count))
        layer_in = layer_in + valid_row * from_time(states)
    upstream = grad_out
    grad_parts = [None] * LAYERS
    for layer_no in range(LAYERS - 1, -1, -1):
        gathered, zhat, inv_std, drive_time, states, count = saved[layer_no]
        decay_wide = jnp.tile(decays[layer_no], clips)
        gain = gains[layer_no]
        previous = jnp.concatenate([jnp.zeros_like(states[:1]), states[:-1]], axis=0)
        pre_time = drive_time + decay_wide[None, :] * previous
        grad_state = to_time(valid_row * upstream)
        start_carry = jnp.zeros((clips * width,), jnp.float32)
        _, grad_pre_time = lax.scan(
            partial(back_step, decay_wide),
            start_carry,
            (grad_state, valid_time, pre_time),
            reverse=True,
            unroll=8,
        )
        decay_local = jnp.sum(
            jnp.sum(grad_pre_time * previous, axis=0).reshape(clips, width), axis=0
        )
        grad_pre = from_time(grad_pre_time)
        gain_local = jnp.sum(grad_pre * zhat, axis=1)
        shift_local = jnp.sum(grad_pre, axis=1)
        grad_gain, grad_shift, grad_decay = lax.psum(
            (gain_local, shift_local, decay_local), "batch"
        )
        grad_pre_norm = (gain * inv_std)[:, None] * (
            grad_pre - valid_row * (grad_shift[:, None] + zhat * grad_gain[:, None]) / count
        )
        weight_local = weight_columns(grad_pre_norm, gathered)
        input_terms = jnp.einsum("jk,jf->kf", weights[layer_no], grad_pre_norm, precision=HIGH)
        input_grad = lax.psum_scatter(input_terms, "neuron", scatter_dimension=0, tiled=True)
        grad_weight = lax.psum(weight_local, "batch")
        upstream = upstream + input_grad
        grad_parts[layer_no] = (grad_weight, grad_gain, grad_shift, grad_decay)
    grad_weights = jnp.stack([grad_parts[layer_no][0] for layer_no in range(LAYERS)])
    grad_gains = jnp.stack([grad_parts[layer_no][1] for layer_no in range(LAYERS)])
    grad_shifts = jnp.stack([grad_parts[layer_no][2] for layer_no in range(LAYERS)])
    grad_decays = jnp.stack([grad_parts[layer_no][3] for layer_no in range(LAYERS)])
    return (layer_in, upstream, grad_weights, grad_gains, grad_shifts, grad_decays, grad_shifts)


def solution(mesh):
    if (mesh.shape["batch"], mesh.shape["neuron"]) == (4, 8):
        cut = Mesh(mesh.devices.reshape(2, 2, 2, 2, 2), ("y", "x", "h", "l", "c"))
        batch, neuron, body = ("y", "x"), ("h", "l", "c"), half_features
    else:
        cut, batch, neuron, body = mesh, "batch", "neuron", split_features
    in_specs = (
        P(neuron, batch),
        P(None, neuron, None),
        P(None, neuron),
        P(None, neuron),
        P(None, neuron),
        P(None, neuron),
        P(batch),
        P(batch, None),
        P(neuron, batch),
    )
    out_specs = (
        P(neuron, batch),
        P(neuron, batch),
        P(None, neuron, None),
        P(None, neuron),
        P(None, neuron),
        P(None, neuron),
        P(None, neuron),
    )
    return jax.shard_map(
        body, mesh=cut, in_specs=in_specs, out_specs=out_specs, check_vma=False
    )
```

```python
from functools import partial
import math

import jax
import jax.numpy as jnp
from jax import lax
from jax.experimental import pallas as pl
from jax.experimental.pallas import tpu as pltpu
from jax.sharding import Mesh, PartitionSpec as P

LAYERS = 2
EPS = 1e-05
HIGH = lax.Precision.HIGHEST
ROOT_TWO = math.sqrt(2.0)
ROOT_TWO_PI = math.sqrt(2.0 * math.pi)
F32 = jnp.float32
BF16 = jnp.bfloat16
LANES = 128
VMEM_LIMIT = 24 * 1024 * 1024
SMEM_SPEC = pl.BlockSpec(memory_space=pltpu.SMEM)
VMEM_SPEC = pl.BlockSpec(memory_space=pltpu.VMEM)


FLIP2 = [(0, 1), (1, 0)]
DIAGONAL = [(0, 3), (1, 2), (2, 1), (3, 0)]


def swap_half(array):
    return lax.ppermute(array, "l", FLIP2)


def after(value, *others):
    return lax.optimization_barrier((value, others))[0]


def split(value):
    high = value.astype(BF16)
    return high, (value - high.astype(F32)).astype(BF16)


def dot(a, b, dims):
    return lax.dot_general(a, b, (dims, ((), ())), preferred_element_type=F32)


NT = ((1,), (1,))
NN = ((1,), (0,))


def in_hbm(array):
    return pltpu.with_memory_space_constraint(array, pltpu.HBM)


def call(body, out_shape, hbm_outs=(), **kwargs):
    if hbm_outs:
        out_shape = [
            pltpu.HBM(a.shape, a.dtype) if i in hbm_outs else a for i, a in enumerate(out_shape)
        ]
    return pl.pallas_call(
        body,
        out_shape=out_shape,
        compiler_params=pltpu.CompilerParams(vmem_limit_bytes=VMEM_LIMIT),
        **kwargs,
    )


def cost(flops, byte_count):
    return pl.CostEstimate(flops=int(flops) // 64, bytes_accessed=int(byte_count) // 64, transcendentals=0)


def pack_body(frames, place_ref, in_ref, near_ref, far_ref, turned):
    slots = in_ref.shape[1]
    for start in range(0, slots, LANES):
        turned[start : start + LANES, :] = in_ref[:, start : start + LANES].T
    for rel in range(4):
        first = pl.multiple_of(place_ref[rel] * frames, 8)
        out = (near_ref, far_ref)[rel // 2]
        out[(rel % 2) * frames : (rel % 2 + 1) * frames, :] = turned[pl.ds(first, frames), :]


def pack(place, array, frames, waits=False):
    width, slots = array.shape
    out = jax.ShapeDtypeStruct((2 * frames, width), F32)
    return call(
        partial(pack_body, frames),
        grid=(1,),
        out_shape=[out, out],
        in_specs=[SMEM_SPEC, pl.BlockSpec((width, slots), lambda i: (0, 0))],
        out_specs=[pl.BlockSpec(out.shape, lambda i: (0, 0))] * 2,
        scratch_shapes=[pltpu.VMEM((slots, width), F32)],
        hbm_outs=(0, 1) if waits else (),
        cost_estimate=cost(0, 8 * width * slots),
        name="pack",
    )(place, in_hbm(array))


def part_spec(part, frames):
    array, i = part
    if i is None:
        return pl.BlockSpec(array.shape, lambda *_: (0,) * array.ndim)
    return pl.BlockSpec((frames, array.shape[1]), lambda *_: (i, 0))


def arrays_of(parts):
    return [array for array, _ in parts]


def unpack_body(frames, place_ref, *refs):
    ins, out_ref, turned = refs[:4], refs[4], refs[5]
    slots = out_ref.shape[1]
    for rel in range(4):
        first = pl.multiple_of(place_ref[rel] * frames, 8)
        turned[pl.ds(first, frames), :] = ins[rel][...]
    for start in range(0, slots, LANES):
        out_ref[:, start : start + LANES] = turned[start : start + LANES, :].T


def unpack(place, parts, frames):
    width = parts[0][0].shape[1]
    slots = 4 * frames
    return call(
        partial(unpack_body, frames),
        grid=(1,),
        out_shape=jax.ShapeDtypeStruct((width, slots), F32),
        in_specs=[SMEM_SPEC] + [part_spec(part, frames) for part in parts],
        out_specs=pl.BlockSpec((width, slots), lambda i: (0, 0)),
        scratch_shapes=[pltpu.VMEM((slots, width), F32)],
        cost_estimate=cost(0, 8 * width * slots),
        name="unpack",
    )(place, *arrays_of(parts))


def merge_body(kept_ref, come_ref, out_ref):
    frames, columns = kept_ref.shape
    width = columns // 2
    for i in range(2):
        some = slice(i * width, (i + 1) * width)
        out_ref[i * frames : (i + 1) * frames, :] = kept_ref[:, some] + come_ref[:, some]


def merge(kept, half, come):
    frames, columns = come.shape
    return call(
        merge_body,
        grid=(1,),
        out_shape=jax.ShapeDtypeStruct((2 * frames, columns // 2), F32),
        in_specs=[
            pl.BlockSpec((frames, columns), lambda i: (0, half)),
            pl.BlockSpec((frames, columns), lambda i: (0, 0)),
        ],
        out_specs=pl.BlockSpec((2 * frames, columns // 2), lambda i: (0, 0)),
        cost_estimate=cost(0, 12 * frames * columns),
        name="merge",
    )(kept, come)


def spread_of(parts, width):
    spots, row, column = [], 0, 0
    for array, _ in parts:
        spots.append((row, column))
        if array.shape[1] == width:
            column += width
        else:
            row += array.shape[0]
    return spots


def project_body(n_parts, spots, with_acc, with_stats, with_params, flat, cols_ref, place_ref, *refs):
    del cols_ref
    parts, refs = refs[:n_parts], refs[n_parts:]
    weights, refs = refs[:10], refs[10:]
    if with_acc:
        acc_ref, refs = refs[0], refs[1:]
    if with_stats:
        valid_ref, refs = refs[0], refs[1:]
    if with_params:
        params_ref, refs = refs[0], refs[1:]
    out_ref, refs = refs[0], refs[1:]
    if with_stats:
        stats_ref, refs = refs[0], refs[1:]
    if flat:
        flat_ref, refs = refs[0], refs[1:]
    x_high, x_low, far_ref = refs
    step = pl.program_id(0)
    width = x_high.shape[2]

    @pl.when(step == 0)
    def _():
        for (row, column), part in zip(spots, parts):
            rows, columns = part.shape
            for start in range(0, columns, width):
                rel = (column + start) // width
                high, low = split(part[:, start : start + width])
                x_high[rel, row : row + rows, :] = high
                x_low[rel, row : row + rows, :] = low
            if flat:
                flat_ref[row : row + rows, column : column + columns] = part[...]
        if with_acc:
            out_ref[...] = acc_ref[...]
        else:
            out_ref[...] = jnp.zeros_like(out_ref)

    stacked = jnp.concatenate([x_high[step], x_low[step], x_high[step]], axis=1)
    for block, weight in enumerate(weight_blocks(place_ref, weights, far_ref)):
        w_high, w_low = split(weight)
        columns = slice(block * width, (block + 1) * width)
        out_ref[:, columns] += dot(stacked, jnp.concatenate([w_high, w_high, w_low], axis=1), NT)

    if with_stats:

        @pl.when(step == pl.num_programs(0) - 1)
        def _():
            valid = valid_ref[...]
            own = jnp.sum(valid, axis=0, keepdims=True)
            per = width // LANES
            for row in range(out_ref.shape[1] // LANES):
                z = out_ref[:, row * LANES : (row + 1) * LANES]
                total = jnp.sum(valid * z, axis=0, keepdims=True)
                centred = valid * (z - total / own)
                squares = jnp.sum(centred * centred, axis=0, keepdims=True)
                at = place_ref[row // per] * per + row % per
                stats_ref[0, pl.ds(at, 1), :] = total
                stats_ref[1, pl.ds(at, 1), :] = squares
                stats_ref[2, pl.ds(at, 1), :] = own
            if with_params:
                rest = params_ref.shape[0] - 8
                stats_ref[3] = params_ref[:8, :]
                stats_ref[4] = jnp.zeros_like(stats_ref[4])
                stats_ref[4, :rest, :] = params_ref[8:, :]


def weight_specs(weights, layer, pairs=2):
    width = weights[0].shape[1]
    specs = []
    for weight in weights:
        if weight.ndim == 3:
            specs.append(
                pl.BlockSpec((1, width, pairs * width), lambda s, cols, *_: (layer, 0, cols[s]))
            )
        else:
            rows = weight.shape[0]
            specs.append(pl.BlockSpec((rows, pairs * width), lambda s, cols, *_: (0, cols[s])))
    return specs


def far_scratch(weights, pairs=2):
    width = weights[0].shape[1]
    return pltpu.VMEM((2, width, pairs * width), F32)


def weight_blocks(place_ref, refs, far_ref):
    for i in range(2):
        for rel, piece in enumerate(refs[2 + 4 * i : 6 + 4 * i]):
            rows = piece.shape[0]
            row = 2 * (place_ref[4] ^ (rel // 2)) + (place_ref[5] ^ (rel % 2))
            far_ref[i, pl.ds(pl.multiple_of(row * rows, rows), rows), :] = piece[...]
    return [refs[0][0], refs[1][0], far_ref[0], far_ref[1]]


def project(
    columns, place, frames, parts, weights, layer, acc=None, valid=None, params=None, flat=False
):
    width = weights[0].shape[-2]
    full = pl.BlockSpec(memory_space=pltpu.VMEM)
    in_specs = [part_spec(part, frames) for part in parts]
    in_specs += weight_specs(weights, layer, 1)
    operands = arrays_of(parts) + [in_hbm(w) for w in weights]
    array = jax.ShapeDtypeStruct((frames, 4 * width), F32)
    array_spec = pl.BlockSpec((frames, 4 * width), lambda s, cols, place: (0, 0))
    out_shape, out_specs = [array], [array_spec]
    if acc is not None:
        in_specs.append(full)
        operands.append(acc)
    if valid is not None:
        in_specs.append(full)
        operands.append(valid)
        stats = (3 if params is None else 5, 4 * width // LANES, LANES)
        out_shape.append(jax.ShapeDtypeStruct(stats, F32))
        out_specs.append(pl.BlockSpec(stats, lambda s, cols, place: (0, 0, 0)))
    if params is not None:
        in_specs.append(full)
        operands.append(params)
    if flat:
        out_shape.append(array)
        out_specs.append(array_spec)
    return call(
        partial(
            project_body,
            len(parts),
            spread_of(parts, width),
            acc is not None,
            valid is not None,
            params is not None,
            flat,
        ),
        grid_spec=pltpu.PrefetchScalarGridSpec(
            num_scalar_prefetch=2,
            grid=(4,),
            in_specs=in_specs,
            out_specs=out_specs,
            scratch_shapes=[pltpu.VMEM((4, frames, width), BF16)] * 2 + [far_scratch(weights, 1)],
        ),
        out_shape=out_shape,
        hbm_outs=((1,) if valid is None else (0, 2)) if flat else (),
        cost_estimate=cost(2 * 3 * frames * 16 * width * width, 4 * 16 * width * width),
        name="project",
    )(columns, place, *operands)


def to_relative(place_ref, spread, rows_ref, value, slot):
    per = value.shape[0] // 4
    spread[...] = value
    for rel in range(4):
        first = place_ref[rel] * per
        for row in range(per):
            rows_ref[slot, rel * per + row : rel * per + row + 1, :] = spread[
                pl.ds(first + row, 1), :
            ]


def tree(values):
    while len(values) > 1:
        values = [a + b for a, b in zip(values[::2], values[1::2])]
    return values[0]


def norm_terms(stats_ref):
    step = stats_ref.shape[0] // 16
    each = [[stats_ref[i] for i in range(slot, stats_ref.shape[0], step)] for slot in range(3)]
    totals, squares, owns = each
    count = tree(owns)
    mean = tree(totals) / count
    away = [total / own - mean for total, own in zip(totals, owns)]
    spread = tree([s + n * a * a for s, n, a in zip(squares, owns, away)])
    return count, mean, lax.rsqrt(spread / count + EPS)


def recur_body(n_parts, spots, last, layer, spread_params, place_ref, gate_ref, z_ref, stats_ref, params_ref, valid_ref, *refs):
    parts, refs = refs[:n_parts], refs[n_parts:]
    outs, refs = refs[: 1 + 2 * last], refs[1 + 2 * last :]
    if spread_params:
        state_ref, slope_ref, params_out, rows, spread, drive_s, state_s, slope_s = refs
    else:
        state_ref, slope_ref, rows, spread, drive_s, state_s, slope_s = refs
    frames = z_ref.shape[0]
    blocks = z_ref.shape[1] // LANES
    per = blocks // 4
    if spread_params:
        for rel in range(4):
            first = place_ref[rel] * (stats_ref.shape[0] // 16)
            for row in range(LAYERS * 3 * per):
                params_out[row // per, rel * per + row % per : rel * per + row % per + 1, :] = (
                    stats_ref[first + 3 + row // 8, row % 8 : row % 8 + 1, :]
                )
        params = [params_out[3 * layer + i] for i in range(3)]
    else:
        params = [params_ref[3 * layer + i] for i in range(3)]
    _, mean, inv_std = norm_terms(stats_ref)
    to_relative(place_ref, spread, rows, mean, 0)
    to_relative(place_ref, spread, rows, inv_std, 1)
    rows[1] = rows[1] * params[0]
    rows[2] = params[1]
    decay = params[2]
    for row in range(blocks):
        z = z_ref[:, row * LANES : (row + 1) * LANES]
        drive_s[row * frames : (row + 1) * frames, :] = (
            z - rows[0, row : row + 1, :]
        ) * rows[1, row : row + 1, :] + rows[2, row : row + 1, :]

    def step(t, state):
        at = pl.ds(t, blocks, stride=frames)
        pre = drive_s[at, :] + decay * state
        half = 0.5 + 0.5 * lax.erf(pre * (1.0 / ROOT_TWO))
        gate = gate_ref[t] > 0.0
        slope = half + pre * jnp.exp(-0.5 * pre * pre) * (1.0 / ROOT_TWO_PI)
        state = jnp.where(gate, pre * half, state)
        state_s[at, :] = state
        slope_s[at, :] = jnp.where(gate, slope, 0.0)
        return state

    lax.fori_loop(0, frames, step, jnp.zeros((blocks, LANES), F32), unroll=8)
    valid = valid_ref[...]
    for row in range(blocks):
        lanes = slice(row * LANES, (row + 1) * LANES)
        state = state_s[row * frames : (row + 1) * frames, :]
        state_ref[:, lanes] = state
        slope_ref[:, lanes] = slope_s[row * frames : (row + 1) * frames, :]
        for (top, column), part in zip(spots, parts):
            if column <= row * LANES < column + part.shape[1]:
                x = part[:, row * LANES - column : (row + 1) * LANES - column]
                some = slice(top, top + part.shape[0])
                value = x + valid[some] * state[some]
                if last:
                    rel, at = divmod(row * LANES, outs[0].shape[1])
                    base = top + frames * (rel == 1)
                    out = outs[max(rel - 1, 0)]
                    out[base : base + part.shape[0], at : at + LANES] = value
                else:
                    outs[0][top : top + part.shape[0], lanes] = value


def recur(layer, place, gate, z, stats, params, valid, parts, last):
    frames, features = z.shape
    width = features // 4
    blocks = features // LANES
    whole = lambda array: pl.BlockSpec(array.shape, lambda i: (0,) * array.ndim)
    full = jax.ShapeDtypeStruct((frames, features), F32)
    piece = jax.ShapeDtypeStruct((frames, width), F32)
    outs = [jax.ShapeDtypeStruct((2 * frames, width), F32), piece, piece] if last else [full]
    out_shape = outs + [full, full]
    spread_params = params is None
    if spread_params:
        out_shape.append(jax.ShapeDtypeStruct((3 * LAYERS, blocks, LANES), F32))
        params = valid
    return call(
        partial(recur_body, len(parts), spread_of(parts, width), last, layer, spread_params),
        grid=(1,),
        in_specs=[SMEM_SPEC, SMEM_SPEC]
        + [whole(a) for a in (z, stats, params, valid)]
        + [part_spec(part, frames) for part in parts],
        out_specs=[whole(s) for s in out_shape],
        out_shape=out_shape,
        scratch_shapes=[
            pltpu.VMEM((3, blocks, LANES), F32),
            pltpu.VMEM((blocks, LANES), F32),
        ]
        + [pltpu.VMEM((blocks * frames, LANES), F32)] * 3,
        hbm_outs=() if last else (1, 2),
        cost_estimate=cost(100 * frames * features, 20 * frames * features),
        name="recur",
    )(place, gate, z if last else in_hbm(z), stats, params, valid, *arrays_of(parts))


def back_body(n_parts, spots, n_state, layer, place_ref, gate_ref, z_ref, stats_ref, params_ref, *refs):
    parts, refs = refs[:n_parts], refs[n_parts:]
    states, refs = refs[:n_state], refs[n_state:]
    slopes, refs = refs[:n_state], refs[n_state:]
    grad_ref, sums_ref, rows, spread, up_s, state_s, slope_s = refs
    frames = z_ref.shape[0]
    blocks = z_ref.shape[1] // LANES
    tall = frames + 8
    _, mean, inv_std = norm_terms(stats_ref)
    to_relative(place_ref, spread, rows, mean, 0)
    to_relative(place_ref, spread, rows, inv_std, 1)
    for row in range(blocks):
        lanes = slice(row * LANES, (row + 1) * LANES)
        base = row * frames
        up = None
        for (top, column), part in zip(spots, parts):
            if column <= row * LANES < column + part.shape[1] and part.shape[0] == frames:
                value = part[:, row * LANES - column : (row + 1) * LANES - column]
                up = value if up is None else up + value
        up_s[base : base + frames, :] = up
        state_s[row * tall : row * tall + 8, :] = jnp.zeros((8, LANES), F32)
        first = 0
        for state, slope in zip(states, slopes):
            some = state.shape[0]
            at = row * tall + 8 + first
            state_s[at : at + some, :] = state[:, lanes]
            slope_s[base + first : base + first + some, :] = slope[:, lanes]
            first += some
    decay = params_ref[3 * layer + 2]

    def step(i, carry):
        t = frames - 1 - i
        at = pl.ds(t, blocks, stride=frames)
        slope = slope_s[at, :]
        gate = gate_ref[t]
        total = gate * up_s[at, :] + carry
        up_s[at, :] = total * slope
        return total * (slope * decay + (1.0 - gate))

    lax.fori_loop(0, frames, step, jnp.zeros((blocks, LANES), F32), unroll=8)
    per = blocks // 4
    for row in range(blocks):
        lanes = slice(row * LANES, (row + 1) * LANES)
        base = row * frames
        grad = up_s[base : base + frames, :]
        grad_ref[:, lanes] = grad
        zhat = (z_ref[:, lanes] - rows[0, row : row + 1, :]) * rows[1, row : row + 1, :]
        before = state_s[row * tall + 7 : row * tall + 7 + frames, :]
        at = place_ref[row // per] * per + row % per
        for slot, value in enumerate((grad * zhat, grad, grad * before)):
            sums_ref[slot, pl.ds(at, 1), :] = jnp.sum(value, axis=0, keepdims=True)


def spots_of_sum(parts, width):
    spots, column = [], 0
    for array, _ in parts:
        spots.append((0, column % (4 * width)))
        column += array.shape[1]
    return spots


def back(layer, place, gate, z, stats, params, ups, states, slopes):
    frames, features = z.shape
    width = features // 4
    blocks = features // LANES
    whole = lambda array: pl.BlockSpec(array.shape, lambda i: (0,) * array.ndim)
    out_shape = [
        jax.ShapeDtypeStruct((frames, features), F32),
        jax.ShapeDtypeStruct((3, blocks, LANES), F32),
    ]
    if layer < LAYERS - 1:
        z, states, slopes = in_hbm(z), [in_hbm(a) for a in states], [in_hbm(a) for a in slopes]
    return call(
        partial(back_body, len(ups), spots_of_sum(ups, width), len(states), layer),
        grid=(1,),
        in_specs=[SMEM_SPEC] * 2
        + [whole(a) for a in (z, stats, params)]
        + [part_spec(up, frames) for up in ups]
        + [whole(a) for a in (*states, *slopes)],
        out_specs=[whole(a) for a in out_shape],
        out_shape=out_shape,
        scratch_shapes=[
            pltpu.VMEM((2, blocks, LANES), F32),
            pltpu.VMEM((blocks, LANES), F32),
            pltpu.VMEM((blocks * frames, LANES), F32),
            pltpu.VMEM((blocks * (frames + 8), LANES), F32),
            pltpu.VMEM((blocks * frames, LANES), F32),
        ],
        cost_estimate=cost(30 * frames * features, 20 * frames * features),
        name="back",
    )(place, gate, z, stats, params, *arrays_of(ups), *states, *slopes)


def input_terms(high_s, low_s, weights):
    left, right = [], []
    for block, weight in enumerate(weights):
        w_high, w_low = split(weight)
        left += [high_s[block], low_s[block], high_s[block]]
        right += [w_high, w_high, w_low]
    return dot(jnp.concatenate(left, axis=1), jnp.concatenate(right, axis=0), NN)


def norm_back_body(split_terms, layer, cols_ref, place_ref, grad_ref, z_ref, params_ref, valid_ref, stats_ref, sums_ref, *refs):
    del cols_ref
    weights, refs = refs[:10], refs[10:]
    if split_terms:
        out_ref, leave_ref, near_term_ref, far_term_ref, sums_out_ref, *refs = refs
        term_refs, starts = (far_term_ref, near_term_ref), (0, 0)
    else:
        out_ref, leave_ref, term_ref, sums_out_ref, *refs = refs
        term_refs, starts = (term_ref, term_ref), (2 * grad_ref.shape[1] // 4, 0)
    rows, spread, high_s, low_s, far_ref = refs
    blocks = z_ref.shape[1] // LANES
    width = high_s.shape[2]
    per = width // LANES

    @pl.when(pl.program_id(0) == 0)
    def _():
        count, mean, inv_std = norm_terms(stats_ref)
        to_relative(place_ref, spread, rows, mean, 0)
        to_relative(place_ref, spread, rows, inv_std, 1)
        rows[2] = rows[1] * params_ref[3 * layer]
        sums = tree([sums_ref[i : i + 3] for i in range(0, sums_ref.shape[0], 3)])
        sums_out_ref[...] = sums
        to_relative(place_ref, spread, rows, sums[0] / count, 3)
        to_relative(place_ref, spread, rows, sums[1] / count, 4)
        valid = valid_ref[...]
        for row in range(blocks):
            lanes = slice(row * LANES, (row + 1) * LANES)
            one = lambda slot: rows[slot, row : row + 1, :]
            zhat = (z_ref[:, lanes] - one(0)) * one(1)
            value = one(2) * (grad_ref[:, lanes] - valid * (one(4) + zhat * one(3)))
            out_ref[:, lanes] = value
            if (row // per) % 2:
                at = (row // per // 2) * width + (row % per) * LANES
                leave_ref[:, at : at + LANES] = value
            high, low = split(value)
            inner = slice((row % per) * LANES, (row % per + 1) * LANES)
            high_s[row // per, :, inner] = high
            low_s[row // per, :, inner] = low

    value = input_terms(high_s, low_s, weight_blocks(place_ref, weights, far_ref))
    for step, (term_ref, first) in enumerate(zip(term_refs, starts)):

        @pl.when(pl.program_id(0) == step)
        def _():
            for pair in range(2):
                at = pl.multiple_of(((place_ref[0] & 1) ^ pair) * width, width)
                term_ref[:, pl.ds(first + at, width)] = value[
                    :, pair * width : (pair + 1) * width
                ]


def norm_back(columns, place, grad, z, params, valid, stats, sums, weights, layer, split_terms):
    frames, features = z.shape
    width = features // 4
    blocks = features // LANES
    whole = lambda array: pl.BlockSpec(array.shape, lambda s, cols, place: (0,) * array.ndim)
    operands = [grad, z if layer == LAYERS - 1 else in_hbm(z), params, valid, stats, sums]
    full = jax.ShapeDtypeStruct((frames, features), F32)
    half = jax.ShapeDtypeStruct((frames, 2 * width), F32)
    terms = [half, half] if split_terms else [full]
    out_shape = [full, half, *terms, jax.ShapeDtypeStruct((3, blocks, LANES), F32)]
    return call(
        partial(norm_back_body, split_terms, layer),
        grid_spec=pltpu.PrefetchScalarGridSpec(
            num_scalar_prefetch=2,
            grid=(2,),
            in_specs=[whole(a) for a in operands] + weight_specs(weights, layer),
            out_specs=[whole(a) for a in out_shape],
            scratch_shapes=[
                pltpu.VMEM((5, blocks, LANES), F32),
                pltpu.VMEM((blocks, LANES), F32),
                pltpu.VMEM((4, frames, width), BF16),
                pltpu.VMEM((4, frames, width), BF16),
                far_scratch(weights),
            ],
        ),
        out_shape=out_shape,
        cost_estimate=cost(6 * frames * features * features, 4 * features * features),
        name="norm_back",
    )(columns, place, *operands, *[in_hbm(w) for w in weights])


def own_terms_body(n_ups, spots, cols_ref, place_ref, grad_ref, *refs):
    del cols_ref
    ups, refs = refs[:n_ups], refs[n_ups:]
    weights, refs = refs[:10], refs[10:]
    out_ref, high_s, low_s, far_ref = refs
    width = high_s.shape[2]
    step = pl.program_id(0)

    @pl.when(step == 0)
    def _():
        for block in range(4):
            high, low = split(grad_ref[:, block * width : (block + 1) * width])
            high_s[block] = high
            low_s[block] = low

    value = input_terms(high_s, low_s, weight_blocks(place_ref, weights, far_ref))
    for pair in range(2):
        at = pl.multiple_of(((place_ref[0] & 1) ^ pair) * width, width)
        out_ref[:, pl.ds(at, width)] = value[:, pair * width : (pair + 1) * width]
    for half in range(2):

        @pl.when(step == half)
        def _():
            first = 2 * half * width
            for (_, column), up in zip(spots, ups):
                low = max(column, first)
                high = min(column + up.shape[1], first + 2 * width)
                if low < high:
                    out_ref[:, low - first : high - first] += up[:, low - column : high - column]


def own_terms(columns, place, grad, ups, weights, layer):
    frames, features = grad.shape
    width = features // 4
    whole = lambda array: pl.BlockSpec(array.shape, lambda s, cols, place: (0,) * array.ndim)
    step_block = pl.BlockSpec((frames, 2 * width), lambda s, cols, place: (0, s))
    return call(
        partial(own_terms_body, len(ups), spots_of_sum(ups, width)),
        grid_spec=pltpu.PrefetchScalarGridSpec(
            num_scalar_prefetch=2,
            grid=(2,),
            in_specs=[whole(grad)]
            + [part_spec(up, frames) for up in ups]
            + weight_specs(weights, layer),
            out_specs=step_block,
            scratch_shapes=[pltpu.VMEM((4, frames, width), BF16)] * 2 + [far_scratch(weights)],
        ),
        out_shape=jax.ShapeDtypeStruct((frames, features), F32),
        cost_estimate=cost(6 * frames * features * features, 4 * features * features),
        name="own_terms",
    )(columns, place, grad, *arrays_of(ups), *[in_hbm(w) for w in weights])


def prepare_body(n_chunks, lists_ref, *refs):
    del lists_ref
    groups = []
    for _ in range(4):
        groups.append(refs[:n_chunks])
        refs = refs[n_chunks:]
    high_ref, low_ref = refs
    padded = high_ref.shape[0] // 2
    for side in range(2):

        @pl.when(pl.program_id(0) // 4 == side)
        def _():
            for clip in range(2):
                row = clip * padded
                for part in groups[2 * clip + side]:
                    rows = part.shape[0]
                    high, low = split(part[...])
                    high_ref[row : row + rows, :] = high
                    low_ref[row : row + rows, :] = low
                    row += rows
                rest = (clip + 1) * padded - row
                zeros = jnp.zeros((rest, high_ref.shape[1]), BF16)
                high_ref[row : row + rest, :] = zeros
                low_ref[row : row + rest, :] = zeros


def prepare(lists, groups):
    width = groups[0][0].shape[1] // 4
    frames = sum(part.shape[0] for part in groups[0])
    padded = -(-frames // LANES) * LANES
    in_specs = []
    for i, group in enumerate(groups):
        for part in group:
            if i % 2 == 0:
                index = lambda s, cols, flip=i // 2: (0, jnp.minimum(s, 3) ^ flip)
            else:
                index = lambda s, cols, flip=i // 2: (0, jnp.maximum(s - 4, 0) ^ flip)
            in_specs.append(pl.BlockSpec((part.shape[0], width), index))
    out = jax.ShapeDtypeStruct((2 * padded, 8 * width), BF16)
    return call(
        partial(prepare_body, len(groups[0])),
        grid_spec=pltpu.PrefetchScalarGridSpec(
            num_scalar_prefetch=1,
            grid=(8,),
            in_specs=in_specs,
            out_specs=[pl.BlockSpec((2 * padded, width), lambda s, cols: (0, cols[s]))] * 2,
        ),
        out_shape=[out, out],
        hbm_outs=(0, 1),
        cost_estimate=cost(0, 16 * frames * 8 * width),
        name="prepare",
    )(lists, *[in_hbm(part) for group in groups for part in group])


def product(g_high, g_low, x_high, x_low):
    return dot(g_high, x_high, NN) + (dot(g_high, x_low, NN) + dot(g_low, x_high, NN))


def weight_body(turn, place_ref, *refs):
    if turn:
        grad_ref, near_ref, x_high, x_low, kept, sent, g_high, g_low, t_high, t_low = refs

        @pl.when(pl.program_id(0) == 0)
        def _():
            frames, features = grad_ref.shape
            width = features // 4
            rows = width // 4
            padded = t_high.shape[1] // 2
            t_high[...] = jnp.zeros_like(t_high)
            t_low[...] = jnp.zeros_like(t_low)
            for clip in range(2):
                for dh in range(2):
                    if clip == 0:
                        part = grad_ref[:, 2 * dh * width : (2 * dh + 1) * width]
                    else:
                        part = near_ref[:, dh * width : (dh + 1) * width]
                    high, low = split(part.T)
                    at = (
                        slice(dh * width, (dh + 1) * width),
                        slice(clip * padded, clip * padded + frames),
                    )
                    t_high[at] = high
                    t_low[at] = low
            for group in range(8):
                first, second, dh = group // 4, group // 2 % 2, group % 2
                core = place_ref[6]
                y = place_ref[4] ^ (first * core + second * (1 - core))
                x = place_ref[5] ^ (first * (1 - core) + second * core)
                at = pl.multiple_of(dh * width + (2 * y + x) * rows, rows)
                g_high[group * rows : (group + 1) * rows, :] = t_high[pl.ds(at, rows), :]
                g_low[group * rows : (group + 1) * rows, :] = t_low[pl.ds(at, rows), :]

    else:
        g_high, g_low, x_high, x_low, kept, sent = refs
    half = g_high.shape[0] // 2
    value = product(g_high[...], g_low[...], x_high[...], x_low[...])
    kept[...] = value[:half].reshape(kept.shape)
    sent[...] = value[half:].reshape(sent.shape)


def weight_rows(half, place, grads, x_split, width):
    turn = half == 0
    whole = lambda array: pl.BlockSpec(array.shape, lambda s, place: (0,) * array.ndim)
    x_spec = pl.BlockSpec((x_split[0].shape[0], width), lambda s, place: (0, 4 * half + s))
    shape = (2, 2, width // 4, 4 * width)
    out_shape = [jax.ShapeDtypeStruct(shape, F32)] * 2
    out_specs = [pl.BlockSpec(shape[:3] + (width,), lambda s, place: (0, 0, 0, s))] * 2
    scratch = []
    if turn:
        turned = (2 * width, x_split[0].shape[0])
        out_shape += [jax.ShapeDtypeStruct(turned, BF16)] * 2
        out_specs += [whole(out_shape[-1])] * 2
        scratch = [pltpu.VMEM(turned, BF16)] * 2
    return call(
        partial(weight_body, turn),
        grid_spec=pltpu.PrefetchScalarGridSpec(
            num_scalar_prefetch=1,
            grid=(4,),
            in_specs=[whole(a) for a in grads] + [x_spec] * 2,
            out_specs=out_specs,
            scratch_shapes=scratch,
        ),
        out_shape=out_shape,
        cost_estimate=cost(12 * x_split[0].shape[0] * width * 4 * width, 4 * 8 * width * width),
        name="weight_rows",
    )(place, *grads, *[in_hbm(x) for x in x_split])


def step_body(n, cut, *refs):
    ins, outs = refs[: 2 * n], refs[2 * n :]
    columns = outs[0].shape[-1]
    column = 0
    for i in range(n):
        total = ins[2 * i][...] + ins[2 * i + 1][...]
        for first in range(0, total.shape[-1], columns):
            at = (column + first) % columns
            rest = min(columns - at, total.shape[-1] - first)
            to = (Ellipsis, slice(at, at + rest))
            piece = total[..., first : first + rest]
            out = (column + first) // columns
            if cut:
                outs[2 * out][to] = piece[0]
                outs[2 * out + 1][to] = piece[1]
            else:
                outs[out][to] = piece
        column += total.shape[-1]


def step_of(*pairs, cut=True, halves=1):
    shape = list(pairs[0][0].shape)
    shape[-1] = sum(pair[0].shape[-1] for pair in pairs) // halves
    out = jax.ShapeDtypeStruct(tuple(shape[1:] if cut else shape), F32)
    outs = [out] * (halves * (1 + cut))
    whole = lambda array: pl.BlockSpec(array.shape, lambda i: (0,) * array.ndim)
    operands = [array for pair in pairs for array in pair]
    return call(
        partial(step_body, len(pairs), cut),
        grid=(1,),
        in_specs=[whole(a) for a in operands],
        out_specs=[whole(a) for a in outs],
        out_shape=outs,
        cost_estimate=cost(0, 4 * sum(a.size for a in operands)),
        name="reduction_step",
    )(*operands)


def plane_swap(array, step):
    pairs = []
    for i in range(8):
        over_x = (i % 2 == 0) == (step == 0)
        pairs.append((i, i ^ 2 if over_x else i ^ 4))
    return lax.ppermute(array, ("y", "x", "c"), pairs)


def plane_gather(share, *before):
    first = plane_swap(share, 0)
    second = plane_swap(share, 1)
    return [share, second, first, plane_swap(after(first, *before), 1)]


def assemble_body(groups, place_ref, *refs):
    out_ref = refs[-1]
    core = place_ref[6]
    column = 0
    for group in range(groups):
        rows, columns = refs[4 * group].shape
        for i in range(4):
            first, second = i // 2, i % 2
            y = place_ref[4] ^ (first * core + second * (1 - core))
            x = place_ref[5] ^ (first * (1 - core) + second * core)
            at = pl.multiple_of((2 * y + x) * rows, rows)
            out_ref[0, pl.ds(at, rows), column : column + columns] = refs[4 * group + i][...]
        column += columns


def assemble(place, groups, layer, onto=None):
    pieces = [piece for group in groups for piece in group]
    rows = 4 * pieces[0].shape[0]
    columns = sum(group[0].shape[1] for group in groups)
    aliases, extra, extra_specs = {}, [], []
    if onto is not None:
        aliases, extra = {1 + len(pieces): 0}, [onto]
        extra_specs = [pl.BlockSpec(memory_space=pl.ANY)]
    (out,) = call(
        partial(assemble_body, len(groups)),
        grid=(1,),
        out_shape=[jax.ShapeDtypeStruct((LAYERS, rows, columns), F32)],
        hbm_outs=(0,),
        in_specs=[SMEM_SPEC]
        + [pl.BlockSpec(p.shape, lambda i: (0, 0)) for p in pieces]
        + extra_specs,
        out_specs=[pl.BlockSpec((1, rows, columns), lambda i: (layer, 0, 0))],
        input_output_aliases=aliases,
        cost_estimate=cost(0, 8 * rows * columns),
        name="assemble",
    )(place, *pieces, *extra)
    return out


def half_features(inputs, weights, gains, shifts, decays, biases, lengths, frame_mask, grad_out):
    width, slots = inputs.shape
    clips, frames = frame_mask.shape
    depth = weights.shape[2]
    blocks = 4 * width // LANES
    y, x, h, l, c = (lax.axis_index(name) for name in ("y", "x", "h", "l", "c"))
    b = 2 * y + x
    numbers = [2 * (h ^ (rel // 2)) + (c ^ (rel % 2)) for rel in range(4)] + [y, x, c]
    place = jnp.stack(numbers).astype(jnp.int32)
    own_blocks, other_blocks = (
        jnp.stack(
            [2 * (2 * (h ^ (rel // 2)) + half) + (c ^ (rel % 2)) for rel in range(4)]
        ).astype(jnp.int32)
        for half in (l, 1 - l)
    )
    all_blocks = jnp.concatenate([own_blocks, other_blocks])
    own_columns = jnp.stack([2 * h + l, 2 * (1 - h) + l]).astype(jnp.int32)
    other_columns = jnp.stack([2 * (1 - h) + 1 - l, 2 * h + 1 - l]).astype(jnp.int32)
    rows = width // 4

    clip = 2 * h + c
    seen = lax.dynamic_index_in_dim(frame_mask, clip, 0, keepdims=False)
    length = lax.dynamic_index_in_dim(lengths, clip, 0, keepdims=False)
    moments = jnp.arange(frames, dtype=jnp.int32)
    gate = ((moments < length) & ((seen == 1) | (moments == 0))).astype(F32)
    valid = jnp.broadcast_to(gate[:, None], (frames, LANES))

    def far_share(layer):
        return lax.dynamic_slice(weights, (layer, b * rows, 0), (1, rows, depth))[0]

    def over_h(array):
        return lax.ppermute(array, "h", FLIP2)

    def over_c(array):
        return lax.ppermute(array, "c", FLIP2)

    def over_second(array):
        return plane_swap(array, 1)

    def four_of(near_rows, far_rows):
        return [
            (near_rows, 0),
            (over_c(near_rows), 1),
            (far_rows, 0),
            (over_c(far_rows), 1),
        ]

    def over_x(array):
        return lax.ppermute(array, "x", FLIP2)

    def over_y(array):
        return lax.ppermute(array, "y", FLIP2)

    def far_pieces(share, direct):
        pieces = [share, over_x(share), over_y(share)]
        others = [over_c(piece) for piece in pieces]
        if direct:
            pieces.append(lax.ppermute(share, ("y", "x"), DIAGONAL))
            others.append(over_c(pieces[3]))
        else:
            pieces.append(over_y(pieces[1]))
            others.append(over_x(others[2]))
        return pieces + others

    near = over_c(weights)
    share = far_share(0)
    close, away = pack(place, after(inputs, share), frames)
    share = over_h(share)
    away = over_h(away)
    other_close = swap_half(close)
    up_close, up_away = pack(place, after(grad_out, close), frames, waits=True)
    share = after(share, up_close, valid)
    half_weights = [[weights, near, *far_pieces(share, False)]]
    away = after(away, other_close, half_weights[0][3:5])
    own = four_of(close, away)
    other_away = swap_half(away)
    params = jnp.stack([gains, shifts + biases, decays], axis=1)
    own_params = params.reshape(LAYERS * 3 * width // LANES, LANES)
    params = None

    saved = []
    for layer in range(LAYERS):
        last = layer == LAYERS - 1
        flat = layer == 0
        if layer > 0:
            others = [(swap_half(array), None) for array, _ in own]
        z, *own_flat = project(
            own_blocks, place, frames, own, half_weights[layer], layer, flat=flat
        )
        if flat:
            others = four_of(other_close, after(other_away, z))
        z, stats, *other_flat = project(
            other_blocks,
            place,
            frames,
            others,
            half_weights[layer],
            layer,
            z,
            valid,
            own_params if flat else None,
            flat,
        )
        if last:
            upstream = four_of(up_close, after(up_away, z))
        if flat:
            stats = lax.all_gather(stats, ("h", "c"), tiled=True)
            share = over_h(after(far_share(1), stats))
            stats = lax.all_gather(stats, ("y", "x"), tiled=True)
        else:
            stats = lax.all_gather(stats, ("y", "x"), tiled=True)
            stats = lax.all_gather(stats, ("h", "c"), tiled=True)
        *following, states, slopes = recur(
            layer, place, gate, z, stats, params, valid, own, last
        )
        if flat:
            *following, states, slopes, params = *following, states, slopes
            groups = [own_flat, other_flat]
        else:
            groups = [arrays_of(own), arrays_of(others)]
        groups += [[over_c(after(p, z)) for p in group] for group in groups]
        x_split = prepare(all_blocks, after(groups, slopes)) if flat else None
        if flat:
            up_away = over_h(after(up_away, x_split[0]))
            half_weights.append([weights, near, *far_pieces(after(share, slopes), True)])
        saved.append((groups, x_split, z, stats, states, slopes))
        own = [(array, None) for array in following]
    output, away, diagonal = following
    diagonal = over_c(over_h(diagonal))

    ups = upstream
    results = [None] * LAYERS
    for layer in range(LAYERS - 1, -1, -1):
        groups, x_split, z, stats, states, slopes = saved[layer]
        weight = half_weights[layer]
        grad_pre, sums = back(
            layer, place, gate, z, stats, params, ups, [states], [slopes]
        )
        plane = lax.all_gather(sums, ("y", "x"), tiled=True)
        if layer == 0:
            later, go = step_of(*[(k, after(g, plane)) for k, g in zip(stay, come)])
            plane = after(plane, later)
            go = over_second(go)
        sums = lax.all_gather(plane, ("h", "c"), tiled=True)
        if layer > 0:
            away = over_h(after(away, sums))
        grad_z, leaving, *terms, sums = norm_back(
            other_columns, place, grad_pre, z, params, valid, stats, sums, weight, layer,
            layer == 0,
        )
        leaving = over_c(leaving)
        if layer > 0:
            received = [swap_half(terms[0])]
            x_split = prepare(all_blocks, after(groups, grad_z, diagonal))
        else:
            received = [None, swap_half(terms[1])]
            later, go = step_of((later, after(go, grad_z)))
            leaving = after(leaving, later)
            later = (later, over_h(go))
        *first, g_high, g_low = weight_rows(0, place, (grad_z, leaving), x_split, width)
        turned = (g_high, g_low)
        come = [plane_swap(first[1], 0)]
        if layer > 0:
            turned = after(turned, away)
            output = [(output, 0), (over_c(output), 1), (away, 0), (diagonal, 0)]
        else:
            received[0] = swap_half(after(terms[0], received[1]))
        second = weight_rows(1, place, turned, x_split, width)
        come.append(plane_swap(second[1], 0))
        stay = (first[0], second[0])
        kept = own_terms(own_columns, place, after(grad_z, second[0]), ups, weight, layer)
        ups = [(kept, None)] + [(r, None) for r in received]
        results[layer] = lax.dynamic_index_in_dim(
            sums.reshape(3, 4, width), clip, axis=1, keepdims=False
        )

    away = merge(kept, 1, received[1])
    (later,) = step_of((later[0], after(later[1], away)), cut=False)
    away = over_h(away)
    later_first, later_second = plane_swap(later, 0), plane_swap(later, 1)
    total, go = step_of((stay[0], after(come[0], later_first)), (stay[1], come[1]))
    go = over_second(go)
    later = [later, later_second, later_first, plane_swap(after(later_first, total), 1)]
    far = [(away, 0), (over_c(away), 1)]
    stay0, go0, stay1, go1 = step_of((total, after(go, far[1][0])), halves=2)
    go0, go1 = over_h(go0), over_h(go1)
    output = unpack(place, [(after(array, stay0), i) for array, i in output], frames)
    (share,) = step_of((stay0, after(go0, output)), cut=False)
    gathered = [plane_gather(share)]
    close = merge(kept, 0, after(received[0], share))
    close = [(close, 0), (over_c(close), 1)]
    grad_weights = assemble(place, after([later], close[0][0]), 1)
    (share,) = step_of((stay1, after(go1, close[0][0])), cut=False)
    gathered.append(plane_gather(share))
    grad_in = unpack(place, [(after(array, share), i) for array, i in close + far], frames)
    grad_weights = assemble(place, after(gathered, grad_in), 0, grad_weights)
    sums = jnp.stack(results)
    return (
        output,
        grad_in,
        grad_weights,
        sums[:, 0],
        sums[:, 1],
        sums[:, 2],
        sums[:, 1],
    )


def gelu_slope(value):
    return (
        0.5 * (1.0 + jax.scipy.special.erf(value / ROOT_TWO))
        + value * jnp.exp(-0.5 * value * value) / ROOT_TWO_PI
    )


def recur_step(decay, state, inputs):
    drive_t, valid_t = inputs
    pre = drive_t + decay * state
    state = state + valid_t * (jax.nn.gelu(pre, approximate=False) - state)
    return (state, state)


def back_step(decay, carry, inputs):
    upstream_t, valid_t, pre_t = inputs
    total = upstream_t + carry
    grad_pre = total * valid_t * gelu_slope(pre_t)
    carry = total * (1.0 - valid_t) + grad_pre * decay
    return (carry, grad_pre)


def add_piece(weight, piece):
    return jnp.dot(weight, piece, precision=HIGH, preferred_element_type=jnp.float32)


def weight_columns(grad_pre_norm, piece):
    return jnp.einsum("jf,kf->jk", grad_pre_norm, piece, precision=HIGH)


def split_features(inputs, weights, gains, shifts, decays, biases, lengths, frame_mask, grad_out):
    width, slots = inputs.shape
    clips, frames_len = frame_mask.shape
    frames = jnp.arange(frames_len, dtype=jnp.int32)
    valid_grid = (
        (frames[None, :] < lengths[:, None]) & ((frame_mask == 1) | (frames[None, :] == 0))
    ).astype(jnp.float32)
    valid = valid_grid.reshape(-1)
    valid_row = valid[None, :]
    valid_time = jnp.broadcast_to(valid_grid.T[:, :, None], (frames_len, clips, width)).reshape(
        frames_len, clips * width
    )
    count_local = jnp.sum(valid)

    def to_time(array):
        return jnp.transpose(array.reshape(width, clips, frames_len), (2, 1, 0)).reshape(
            frames_len, clips * width
        )

    def from_time(array):
        return jnp.transpose(array.reshape(frames_len, clips, width), (2, 1, 0)).reshape(
            width, slots
        )

    layer_in = inputs
    saved = []
    for layer_no in range(LAYERS):
        weight = weights[layer_no]
        gathered = lax.all_gather(layer_in, "neuron", axis=0, tiled=True)
        pre_norm = add_piece(weight, gathered)
        first_sum, count = lax.psum((jnp.sum(valid_row * pre_norm, axis=1), count_local), "batch")
        mean = first_sum / count
        centered = pre_norm - mean[:, None]
        var = lax.psum(jnp.sum(valid_row * centered * centered, axis=1), "batch") / count
        inv_std = lax.rsqrt(var + EPS)
        zhat = (pre_norm - mean[:, None]) * inv_std[:, None]
        drive = gains[layer_no][:, None] * zhat + (shifts[layer_no] + biases[layer_no])[:, None]
        drive_time = to_time(drive)
        decay_wide = jnp.tile(decays[layer_no], clips)
        start_state = jnp.zeros((clips * width,), jnp.float32)
        _, states = lax.scan(
            partial(recur_step, decay_wide), start_state, (drive_time, valid_time), unroll=8
        )
        saved.append((gathered, zhat, inv_std, drive_time, states, count))
        layer_in = layer_in + valid_row * from_time(states)
    upstream = grad_out
    grad_parts = [None] * LAYERS
    for layer_no in range(LAYERS - 1, -1, -1):
        gathered, zhat, inv_std, drive_time, states, count = saved[layer_no]
        decay_wide = jnp.tile(decays[layer_no], clips)
        gain = gains[layer_no]
        previous = jnp.concatenate([jnp.zeros_like(states[:1]), states[:-1]], axis=0)
        pre_time = drive_time + decay_wide[None, :] * previous
        grad_state = to_time(valid_row * upstream)
        start_carry = jnp.zeros((clips * width,), jnp.float32)
        _, grad_pre_time = lax.scan(
            partial(back_step, decay_wide),
            start_carry,
            (grad_state, valid_time, pre_time),
            reverse=True,
            unroll=8,
        )
        decay_local = jnp.sum(
            jnp.sum(grad_pre_time * previous, axis=0).reshape(clips, width), axis=0
        )
        grad_pre = from_time(grad_pre_time)
        gain_local = jnp.sum(grad_pre * zhat, axis=1)
        shift_local = jnp.sum(grad_pre, axis=1)
        grad_gain, grad_shift, grad_decay = lax.psum(
            (gain_local, shift_local, decay_local), "batch"
        )
        grad_pre_norm = (gain * inv_std)[:, None] * (
            grad_pre - valid_row * (grad_shift[:, None] + zhat * grad_gain[:, None]) / count
        )
        weight_local = weight_columns(grad_pre_norm, gathered)
        input_terms = jnp.einsum("jk,jf->kf", weights[layer_no], grad_pre_norm, precision=HIGH)
        input_grad = lax.psum_scatter(input_terms, "neuron", scatter_dimension=0, tiled=True)
        grad_weight = lax.psum(weight_local, "batch")
        upstream = upstream + input_grad
        grad_parts[layer_no] = (grad_weight, grad_gain, grad_shift, grad_decay)
    grad_weights = jnp.stack([grad_parts[layer_no][0] for layer_no in range(LAYERS)])
    grad_gains = jnp.stack([grad_parts[layer_no][1] for layer_no in range(LAYERS)])
    grad_shifts = jnp.stack([grad_parts[layer_no][2] for layer_no in range(LAYERS)])
    grad_decays = jnp.stack([grad_parts[layer_no][3] for layer_no in range(LAYERS)])
    return (layer_in, upstream, grad_weights, grad_gains, grad_shifts, grad_decays, grad_shifts)


def solution(mesh):
    if (mesh.shape["batch"], mesh.shape["neuron"]) == (4, 8):
        cut = Mesh(mesh.devices.reshape(2, 2, 2, 2, 2), ("y", "x", "h", "l", "c"))
        batch, neuron, body = ("y", "x"), ("h", "l", "c"), half_features
    else:
        cut, batch, neuron, body = mesh, "batch", "neuron", split_features
    in_specs = (
        P(neuron, batch),
        P(None, neuron, None),
        P(None, neuron),
        P(None, neuron),
        P(None, neuron),
        P(None, neuron),
        P(batch),
        P(batch, None),
        P(neuron, batch),
    )
    out_specs = (
        P(neuron, batch),
        P(neuron, batch),
        P(None, neuron, None),
        P(None, neuron),
        P(None, neuron),
        P(None, neuron),
        P(None, neuron),
    )
    return jax.shard_map(
        body, mesh=cut, in_specs=in_specs, out_specs=out_specs, check_vma=False
    )
```

```python
from functools import partial
import math

import jax
import jax.numpy as jnp
from jax import lax
from jax.experimental import pallas as pl
from jax.experimental.pallas import tpu as pltpu
from jax.sharding import Mesh, PartitionSpec as P

LAYERS = 2
EPS = 1e-05
HIGH = lax.Precision.HIGHEST
ROOT_TWO = math.sqrt(2.0)
ROOT_TWO_PI = math.sqrt(2.0 * math.pi)
F32 = jnp.float32
BF16 = jnp.bfloat16
LANES = 128
VMEM_LIMIT = 24 * 1024 * 1024
SMEM_SPEC = pl.BlockSpec(memory_space=pltpu.SMEM)
VMEM_SPEC = pl.BlockSpec(memory_space=pltpu.VMEM)


FLIP2 = [(0, 1), (1, 0)]
DIAGONAL = [(0, 3), (1, 2), (2, 1), (3, 0)]


def swap_half(array):
    return lax.ppermute(array, "l", FLIP2)


def after(value, *others):
    return lax.optimization_barrier((value, others))[0]


def split(value):
    high = value.astype(BF16)
    return high, (value - high.astype(F32)).astype(BF16)


def dot(a, b, dims):
    return lax.dot_general(a, b, (dims, ((), ())), preferred_element_type=F32)


NT = ((1,), (1,))
NN = ((1,), (0,))


def in_hbm(array):
    return pltpu.with_memory_space_constraint(array, pltpu.HBM)


def call(body, out_shape, hbm_outs=(), **kwargs):
    if hbm_outs:
        out_shape = [
            pltpu.HBM(a.shape, a.dtype) if i in hbm_outs else a for i, a in enumerate(out_shape)
        ]
    return pl.pallas_call(
        body,
        out_shape=out_shape,
        compiler_params=pltpu.CompilerParams(vmem_limit_bytes=VMEM_LIMIT),
        **kwargs,
    )


def cost(flops, byte_count):
    return pl.CostEstimate(flops=int(flops) // 64, bytes_accessed=int(byte_count) // 64, transcendentals=0)


def pack_body(frames, place_ref, in_ref, near_ref, far_ref, turned):
    slots = in_ref.shape[1]
    for start in range(0, slots, LANES):
        turned[start : start + LANES, :] = in_ref[:, start : start + LANES].T
    for rel in range(4):
        first = pl.multiple_of(place_ref[rel] * frames, 8)
        out = (near_ref, far_ref)[rel // 2]
        out[(rel % 2) * frames : (rel % 2 + 1) * frames, :] = turned[pl.ds(first, frames), :]


def pack(place, array, frames, waits=False):
    width, slots = array.shape
    out = jax.ShapeDtypeStruct((2 * frames, width), F32)
    return call(
        partial(pack_body, frames),
        grid=(1,),
        out_shape=[out, out],
        in_specs=[SMEM_SPEC, pl.BlockSpec((width, slots), lambda i: (0, 0))],
        out_specs=[pl.BlockSpec(out.shape, lambda i: (0, 0))] * 2,
        scratch_shapes=[pltpu.VMEM((slots, width), F32)],
        hbm_outs=(0, 1) if waits else (),
        cost_estimate=cost(0, 8 * width * slots),
        name="pack",
    )(place, in_hbm(array))


def part_spec(part, frames):
    array, i = part
    if i is None:
        return pl.BlockSpec(array.shape, lambda *_: (0,) * array.ndim)
    return pl.BlockSpec((frames, array.shape[1]), lambda *_: (i, 0))


def arrays_of(parts):
    return [array for array, _ in parts]


def unpack_body(frames, place_ref, *refs):
    ins, out_ref, turned = refs[:4], refs[4], refs[5]
    slots = out_ref.shape[1]
    for rel in range(4):
        first = pl.multiple_of(place_ref[rel] * frames, 8)
        turned[pl.ds(first, frames), :] = ins[rel][...]
    for start in range(0, slots, LANES):
        out_ref[:, start : start + LANES] = turned[start : start + LANES, :].T


def unpack(place, parts, frames, waited=False):
    width = parts[0][0].shape[1]
    slots = 4 * frames
    return call(
        partial(unpack_body, frames),
        grid=(1,),
        out_shape=jax.ShapeDtypeStruct((width, slots), F32),
        in_specs=[SMEM_SPEC] + [part_spec(part, frames) for part in parts],
        out_specs=pl.BlockSpec((width, slots), lambda i: (0, 0)),
        scratch_shapes=[pltpu.VMEM((slots, width), F32)],
        cost_estimate=cost(0, 8 * width * slots),
        name="unpack",
    )(place, *[in_hbm(a) if waited else a for a in arrays_of(parts)])


def merge_body(kept_ref, come_ref, out_ref):
    frames, columns = kept_ref.shape
    width = columns // 2
    for i in range(2):
        some = slice(i * width, (i + 1) * width)
        out_ref[i * frames : (i + 1) * frames, :] = kept_ref[:, some] + come_ref[:, some]


def merge(kept, half, come):
    frames, columns = come.shape
    return call(
        merge_body,
        grid=(1,),
        out_shape=jax.ShapeDtypeStruct((2 * frames, columns // 2), F32),
        in_specs=[
            pl.BlockSpec((frames, columns), lambda i: (0, half)),
            pl.BlockSpec((frames, columns), lambda i: (0, 0)),
        ],
        out_specs=pl.BlockSpec((2 * frames, columns // 2), lambda i: (0, 0)),
        cost_estimate=cost(0, 12 * frames * columns),
        name="merge",
    )(kept, come)


def spread_of(parts, width):
    spots, row, column = [], 0, 0
    for array, _ in parts:
        spots.append((row, column))
        if array.shape[1] == width:
            column += width
        else:
            row += array.shape[0]
    return spots


def project_body(n_parts, spots, with_acc, with_stats, with_params, flat, cols_ref, place_ref, *refs):
    del cols_ref
    parts, refs = refs[:n_parts], refs[n_parts:]
    weights, refs = refs[:10], refs[10:]
    if with_acc:
        acc_ref, refs = refs[0], refs[1:]
    if with_stats:
        valid_ref, refs = refs[0], refs[1:]
    if with_params:
        params_ref, refs = refs[0], refs[1:]
    out_ref, refs = refs[0], refs[1:]
    if with_stats:
        stats_ref, refs = refs[0], refs[1:]
    if flat:
        flat_ref, refs = refs[0], refs[1:]
    x_high, x_low, far_ref = refs
    step = pl.program_id(0)
    width = x_high.shape[2]

    @pl.when(step == 0)
    def _():
        for (row, column), part in zip(spots, parts):
            rows, columns = part.shape
            for start in range(0, columns, width):
                rel = (column + start) // width
                high, low = split(part[:, start : start + width])
                x_high[rel, row : row + rows, :] = high
                x_low[rel, row : row + rows, :] = low
            if flat:
                flat_ref[row : row + rows, column : column + columns] = part[...]
        if with_acc:
            out_ref[...] = acc_ref[...]
        else:
            out_ref[...] = jnp.zeros_like(out_ref)

    stacked = jnp.concatenate([x_high[step], x_low[step], x_high[step]], axis=1)
    for block, weight in enumerate(weight_blocks(place_ref, weights, far_ref)):
        w_high, w_low = split(weight)
        columns = slice(block * width, (block + 1) * width)
        out_ref[:, columns] += dot(stacked, jnp.concatenate([w_high, w_high, w_low], axis=1), NT)

    if with_stats:

        @pl.when(step == pl.num_programs(0) - 1)
        def _():
            valid = valid_ref[...]
            own = jnp.sum(valid, axis=0, keepdims=True)
            per = width // LANES
            for row in range(out_ref.shape[1] // LANES):
                z = out_ref[:, row * LANES : (row + 1) * LANES]
                total = jnp.sum(valid * z, axis=0, keepdims=True)
                centred = valid * (z - total / own)
                squares = jnp.sum(centred * centred, axis=0, keepdims=True)
                at = place_ref[row // per] * per + row % per
                stats_ref[0, pl.ds(at, 1), :] = total
                stats_ref[1, pl.ds(at, 1), :] = squares
                stats_ref[2, pl.ds(at, 1), :] = own
            if with_params:
                rest = params_ref.shape[0] - 8
                stats_ref[3] = params_ref[:8, :]
                stats_ref[4] = jnp.zeros_like(stats_ref[4])
                stats_ref[4, :rest, :] = params_ref[8:, :]


def weight_specs(weights, layer, pairs=2):
    width = weights[0].shape[1]
    specs = []
    for weight in weights:
        if weight.ndim == 3:
            specs.append(
                pl.BlockSpec((1, width, pairs * width), lambda s, cols, *_: (layer, 0, cols[s]))
            )
        else:
            rows = weight.shape[0]
            specs.append(pl.BlockSpec((rows, pairs * width), lambda s, cols, *_: (0, cols[s])))
    return specs


def far_scratch(weights, pairs=2):
    width = weights[0].shape[1]
    return pltpu.VMEM((2, width, pairs * width), F32)


def weight_blocks(place_ref, refs, far_ref):
    for i in range(2):
        for rel, piece in enumerate(refs[2 + 4 * i : 6 + 4 * i]):
            rows = piece.shape[0]
            row = 2 * (place_ref[4] ^ (rel // 2)) + (place_ref[5] ^ (rel % 2))
            far_ref[i, pl.ds(pl.multiple_of(row * rows, rows), rows), :] = piece[...]
    return [refs[0][0], refs[1][0], far_ref[0], far_ref[1]]


def project(
    columns, place, frames, parts, weights, layer, acc=None, valid=None, params=None, flat=False
):
    width = weights[0].shape[-2]
    full = pl.BlockSpec(memory_space=pltpu.VMEM)
    in_specs = [part_spec(part, frames) for part in parts]
    in_specs += weight_specs(weights, layer, 1)
    operands = arrays_of(parts) + [in_hbm(w) for w in weights]
    array = jax.ShapeDtypeStruct((frames, 4 * width), F32)
    array_spec = pl.BlockSpec((frames, 4 * width), lambda s, cols, place: (0, 0))
    out_shape, out_specs = [array], [array_spec]
    if acc is not None:
        in_specs.append(array_spec)
        operands.append(in_hbm(acc))
    if valid is not None:
        in_specs.append(full)
        operands.append(valid)
        stats = (3 if params is None else 5, 4 * width // LANES, LANES)
        out_shape.append(jax.ShapeDtypeStruct(stats, F32))
        out_specs.append(pl.BlockSpec(stats, lambda s, cols, place: (0, 0, 0)))
    if params is not None:
        in_specs.append(full)
        operands.append(params)
    if flat:
        out_shape.append(array)
        out_specs.append(array_spec)
    return call(
        partial(
            project_body,
            len(parts),
            spread_of(parts, width),
            acc is not None,
            valid is not None,
            params is not None,
            flat,
        ),
        grid_spec=pltpu.PrefetchScalarGridSpec(
            num_scalar_prefetch=2,
            grid=(4,),
            in_specs=in_specs,
            out_specs=out_specs,
            scratch_shapes=[pltpu.VMEM((4, frames, width), BF16)] * 2 + [far_scratch(weights, 1)],
        ),
        out_shape=out_shape,
        hbm_outs=(0, len(out_shape) - 1) if flat else (0,),
        cost_estimate=cost(2 * 3 * frames * 16 * width * width, 4 * 16 * width * width),
        name="project",
    )(columns, place, *operands)


def to_relative(place_ref, spread, rows_ref, value, slot):
    per = value.shape[0] // 4
    spread[...] = value
    for rel in range(4):
        first = place_ref[rel] * per
        for row in range(per):
            rows_ref[slot, rel * per + row : rel * per + row + 1, :] = spread[
                pl.ds(first + row, 1), :
            ]


def tree(values):
    while len(values) > 1:
        values = [a + b for a, b in zip(values[::2], values[1::2])]
    return values[0]


def norm_terms(stats_ref):
    step = stats_ref.shape[0] // 16
    each = [[stats_ref[i] for i in range(slot, stats_ref.shape[0], step)] for slot in range(3)]
    totals, squares, owns = each
    count = tree(owns)
    mean = tree(totals) / count
    away = [total / own - mean for total, own in zip(totals, owns)]
    spread = tree([s + n * a * a for s, n, a in zip(squares, owns, away)])
    return count, mean, lax.rsqrt(spread / count + EPS)


def recur_body(n_parts, spots, last, layer, spread_params, place_ref, gate_ref, z_ref, stats_ref, params_ref, valid_ref, *refs):
    parts, refs = refs[:n_parts], refs[n_parts:]
    outs, refs = refs[: 1 + 2 * last], refs[1 + 2 * last :]
    if spread_params:
        state_ref, slope_ref, params_out, rows, spread, drive_s, state_s, slope_s = refs
    else:
        state_ref, slope_ref, rows, spread, drive_s, state_s, slope_s = refs
    frames = z_ref.shape[0]
    blocks = z_ref.shape[1] // LANES
    per = blocks // 4
    if spread_params:
        for rel in range(4):
            first = place_ref[rel] * (stats_ref.shape[0] // 16)
            for row in range(LAYERS * 3 * per):
                params_out[row // per, rel * per + row % per : rel * per + row % per + 1, :] = (
                    stats_ref[first + 3 + row // 8, row % 8 : row % 8 + 1, :]
                )
        params = [params_out[3 * layer + i] for i in range(3)]
    else:
        params = [params_ref[3 * layer + i] for i in range(3)]
    _, mean, inv_std = norm_terms(stats_ref)
    to_relative(place_ref, spread, rows, mean, 0)
    to_relative(place_ref, spread, rows, inv_std, 1)
    rows[1] = rows[1] * params[0]
    rows[2] = params[1]
    decay = params[2]
    for row in range(blocks):
        z = z_ref[:, row * LANES : (row + 1) * LANES]
        drive_s[row * frames : (row + 1) * frames, :] = (
            z - rows[0, row : row + 1, :]
        ) * rows[1, row : row + 1, :] + rows[2, row : row + 1, :]

    def step(t, state):
        at = pl.ds(t, blocks, stride=frames)
        pre = drive_s[at, :] + decay * state
        half = 0.5 + 0.5 * lax.erf(pre * (1.0 / ROOT_TWO))
        gate = gate_ref[t] > 0.0
        slope = half + pre * jnp.exp(-0.5 * pre * pre) * (1.0 / ROOT_TWO_PI)
        state = jnp.where(gate, pre * half, state)
        state_s[at, :] = state
        slope_s[at, :] = jnp.where(gate, slope, 0.0)
        return state

    lax.fori_loop(0, frames, step, jnp.zeros((blocks, LANES), F32), unroll=8)
    valid = valid_ref[...]
    for row in range(blocks):
        lanes = slice(row * LANES, (row + 1) * LANES)
        state = state_s[row * frames : (row + 1) * frames, :]
        state_ref[:, lanes] = state
        slope_ref[:, lanes] = slope_s[row * frames : (row + 1) * frames, :]
        for (top, column), part in zip(spots, parts):
            if column <= row * LANES < column + part.shape[1]:
                x = part[:, row * LANES - column : (row + 1) * LANES - column]
                some = slice(top, top + part.shape[0])
                value = x + valid[some] * state[some]
                if last:
                    rel, at = divmod(row * LANES, outs[0].shape[1])
                    base = top + frames * (rel == 1)
                    out = outs[max(rel - 1, 0)]
                    out[base : base + part.shape[0], at : at + LANES] = value
                else:
                    outs[0][top : top + part.shape[0], lanes] = value


def recur(layer, place, gate, z, stats, params, valid, parts, last):
    frames, features = z.shape
    width = features // 4
    blocks = features // LANES
    whole = lambda array: pl.BlockSpec(array.shape, lambda i: (0,) * array.ndim)
    full = jax.ShapeDtypeStruct((frames, features), F32)
    piece = jax.ShapeDtypeStruct((frames, width), F32)
    outs = [jax.ShapeDtypeStruct((2 * frames, width), F32), piece, piece] if last else [full]
    out_shape = outs + [full, full]
    spread_params = params is None
    if spread_params:
        out_shape.append(jax.ShapeDtypeStruct((3 * LAYERS, blocks, LANES), F32))
        params = valid
    return call(
        partial(recur_body, len(parts), spread_of(parts, width), last, layer, spread_params),
        grid=(1,),
        in_specs=[SMEM_SPEC, SMEM_SPEC]
        + [whole(a) for a in (z, stats, params, valid)]
        + [part_spec(part, frames) for part in parts],
        out_specs=[whole(s) for s in out_shape],
        out_shape=out_shape,
        scratch_shapes=[
            pltpu.VMEM((3, blocks, LANES), F32),
            pltpu.VMEM((blocks, LANES), F32),
        ]
        + [pltpu.VMEM((blocks * frames, LANES), F32)] * 3,
        hbm_outs=(0, 1, 2, 3, 4) if last else (1, 2),
        cost_estimate=cost(100 * frames * features, 20 * frames * features),
        name="recur",
    )(place, gate, in_hbm(z), stats, params, valid, *[in_hbm(a) for a in arrays_of(parts)])


def back_body(n_parts, spots, n_state, layer, place_ref, gate_ref, z_ref, stats_ref, params_ref, *refs):
    parts, refs = refs[:n_parts], refs[n_parts:]
    states, refs = refs[:n_state], refs[n_state:]
    slopes, refs = refs[:n_state], refs[n_state:]
    grad_ref, sums_ref, rows, spread, up_s, state_s, slope_s = refs
    frames = z_ref.shape[0]
    blocks = z_ref.shape[1] // LANES
    tall = frames + 8
    _, mean, inv_std = norm_terms(stats_ref)
    to_relative(place_ref, spread, rows, mean, 0)
    to_relative(place_ref, spread, rows, inv_std, 1)
    for row in range(blocks):
        lanes = slice(row * LANES, (row + 1) * LANES)
        base = row * frames
        up = None
        for (top, column), part in zip(spots, parts):
            if column <= row * LANES < column + part.shape[1] and part.shape[0] == frames:
                value = part[:, row * LANES - column : (row + 1) * LANES - column]
                up = value if up is None else up + value
        up_s[base : base + frames, :] = up
        state_s[row * tall : row * tall + 8, :] = jnp.zeros((8, LANES), F32)
        first = 0
        for state, slope in zip(states, slopes):
            some = state.shape[0]
            at = row * tall + 8 + first
            state_s[at : at + some, :] = state[:, lanes]
            slope_s[base + first : base + first + some, :] = slope[:, lanes]
            first += some
    decay = params_ref[3 * layer + 2]

    def step(i, carry):
        t = frames - 1 - i
        at = pl.ds(t, blocks, stride=frames)
        slope = slope_s[at, :]
        gate = gate_ref[t]
        total = gate * up_s[at, :] + carry
        up_s[at, :] = total * slope
        return total * (slope * decay + (1.0 - gate))

    lax.fori_loop(0, frames, step, jnp.zeros((blocks, LANES), F32), unroll=8)
    per = blocks // 4
    for row in range(blocks):
        lanes = slice(row * LANES, (row + 1) * LANES)
        base = row * frames
        grad = up_s[base : base + frames, :]
        grad_ref[:, lanes] = grad
        zhat = (z_ref[:, lanes] - rows[0, row : row + 1, :]) * rows[1, row : row + 1, :]
        before = state_s[row * tall + 7 : row * tall + 7 + frames, :]
        at = place_ref[row // per] * per + row % per
        for slot, value in enumerate((grad * zhat, grad, grad * before)):
            sums_ref[slot, pl.ds(at, 1), :] = jnp.sum(value, axis=0, keepdims=True)


def spots_of_sum(parts, width):
    spots, column = [], 0
    for array, _ in parts:
        spots.append((0, column % (4 * width)))
        column += array.shape[1]
    return spots


def back(layer, place, gate, z, stats, params, ups, states, slopes):
    frames, features = z.shape
    width = features // 4
    blocks = features // LANES
    whole = lambda array: pl.BlockSpec(array.shape, lambda i: (0,) * array.ndim)
    out_shape = [
        jax.ShapeDtypeStruct((frames, features), F32),
        jax.ShapeDtypeStruct((3, blocks, LANES), F32),
    ]
    z, states, slopes = in_hbm(z), [in_hbm(a) for a in states], [in_hbm(a) for a in slopes]
    return call(
        partial(back_body, len(ups), spots_of_sum(ups, width), len(states), layer),
        grid=(1,),
        in_specs=[SMEM_SPEC] * 2
        + [whole(a) for a in (z, stats, params)]
        + [part_spec(up, frames) for up in ups]
        + [whole(a) for a in (*states, *slopes)],
        out_specs=[whole(a) for a in out_shape],
        out_shape=out_shape,
        scratch_shapes=[
            pltpu.VMEM((2, blocks, LANES), F32),
            pltpu.VMEM((blocks, LANES), F32),
            pltpu.VMEM((blocks * frames, LANES), F32),
            pltpu.VMEM((blocks * (frames + 8), LANES), F32),
            pltpu.VMEM((blocks * frames, LANES), F32),
        ],
        cost_estimate=cost(30 * frames * features, 20 * frames * features),
        name="back",
    )(place, gate, z, stats, params, *arrays_of(ups), *states, *slopes)


def input_terms(high_s, low_s, weights):
    left, right = [], []
    for block, weight in enumerate(weights):
        w_high, w_low = split(weight)
        left += [high_s[block], low_s[block], high_s[block]]
        right += [w_high, w_high, w_low]
    return dot(jnp.concatenate(left, axis=1), jnp.concatenate(right, axis=0), NN)


def norm_back_body(split_terms, layer, cols_ref, place_ref, grad_ref, z_ref, params_ref, valid_ref, stats_ref, sums_ref, *refs):
    del cols_ref
    weights, refs = refs[:10], refs[10:]
    if split_terms:
        out_ref, leave_ref, near_term_ref, far_term_ref, sums_out_ref, *refs = refs
        term_refs, starts = (far_term_ref, near_term_ref), (0, 0)
    else:
        out_ref, leave_ref, term_ref, sums_out_ref, *refs = refs
        term_refs, starts = (term_ref, term_ref), (2 * grad_ref.shape[1] // 4, 0)
    rows, spread, high_s, low_s, far_ref = refs
    blocks = z_ref.shape[1] // LANES
    width = high_s.shape[2]
    per = width // LANES

    @pl.when(pl.program_id(0) == 0)
    def _():
        count, mean, inv_std = norm_terms(stats_ref)
        to_relative(place_ref, spread, rows, mean, 0)
        to_relative(place_ref, spread, rows, inv_std, 1)
        rows[2] = rows[1] * params_ref[3 * layer]
        sums = tree([sums_ref[i : i + 3] for i in range(0, sums_ref.shape[0], 3)])
        sums_out_ref[...] = sums
        to_relative(place_ref, spread, rows, sums[0] / count, 3)
        to_relative(place_ref, spread, rows, sums[1] / count, 4)
        valid = valid_ref[...]
        for row in range(blocks):
            lanes = slice(row * LANES, (row + 1) * LANES)
            one = lambda slot: rows[slot, row : row + 1, :]
            zhat = (z_ref[:, lanes] - one(0)) * one(1)
            value = one(2) * (grad_ref[:, lanes] - valid * (one(4) + zhat * one(3)))
            out_ref[:, lanes] = value
            if (row // per) % 2:
                at = (row // per // 2) * width + (row % per) * LANES
                leave_ref[:, at : at + LANES] = value
            high, low = split(value)
            inner = slice((row % per) * LANES, (row % per + 1) * LANES)
            high_s[row // per, :, inner] = high
            low_s[row // per, :, inner] = low

    value = input_terms(high_s, low_s, weight_blocks(place_ref, weights, far_ref))
    for step, (term_ref, first) in enumerate(zip(term_refs, starts)):

        @pl.when(pl.program_id(0) == step)
        def _():
            for pair in range(2):
                at = pl.multiple_of(((place_ref[0] & 1) ^ pair) * width, width)
                term_ref[:, pl.ds(first + at, width)] = value[
                    :, pair * width : (pair + 1) * width
                ]


def norm_back(columns, place, grad, z, params, valid, stats, sums, weights, layer, split_terms):
    frames, features = z.shape
    width = features // 4
    blocks = features // LANES
    whole = lambda array: pl.BlockSpec(array.shape, lambda s, cols, place: (0,) * array.ndim)
    operands = [grad, in_hbm(z), params, valid, stats, sums]
    full = jax.ShapeDtypeStruct((frames, features), F32)
    half = jax.ShapeDtypeStruct((frames, 2 * width), F32)
    terms = [half, half] if split_terms else [full]
    out_shape = [full, half, *terms, jax.ShapeDtypeStruct((3, blocks, LANES), F32)]
    return call(
        partial(norm_back_body, split_terms, layer),
        grid_spec=pltpu.PrefetchScalarGridSpec(
            num_scalar_prefetch=2,
            grid=(2,),
            in_specs=[whole(a) for a in operands] + weight_specs(weights, layer),
            out_specs=[whole(a) for a in out_shape],
            scratch_shapes=[
                pltpu.VMEM((5, blocks, LANES), F32),
                pltpu.VMEM((blocks, LANES), F32),
                pltpu.VMEM((4, frames, width), BF16),
                pltpu.VMEM((4, frames, width), BF16),
                far_scratch(weights),
            ],
        ),
        out_shape=out_shape,
        hbm_outs=(0,),
        cost_estimate=cost(6 * frames * features * features, 4 * features * features),
        name="norm_back",
    )(columns, place, *operands, *[in_hbm(w) for w in weights])


def own_terms_body(n_ups, spots, cols_ref, place_ref, grad_ref, *refs):
    del cols_ref
    ups, refs = refs[:n_ups], refs[n_ups:]
    weights, refs = refs[:10], refs[10:]
    out_ref, high_s, low_s, far_ref = refs
    width = high_s.shape[2]
    step = pl.program_id(0)

    @pl.when(step == 0)
    def _():
        for block in range(4):
            high, low = split(grad_ref[:, block * width : (block + 1) * width])
            high_s[block] = high
            low_s[block] = low

    value = input_terms(high_s, low_s, weight_blocks(place_ref, weights, far_ref))
    for pair in range(2):
        at = pl.multiple_of(((place_ref[0] & 1) ^ pair) * width, width)
        out_ref[:, pl.ds(at, width)] = value[:, pair * width : (pair + 1) * width]
    for half in range(2):

        @pl.when(step == half)
        def _():
            first = 2 * half * width
            for (_, column), up in zip(spots, ups):
                low = max(column, first)
                high = min(column + up.shape[1], first + 2 * width)
                if low < high:
                    out_ref[:, low - first : high - first] += up[:, low - column : high - column]


def own_terms(columns, place, grad, ups, weights, layer):
    frames, features = grad.shape
    width = features // 4
    whole = lambda array: pl.BlockSpec(array.shape, lambda s, cols, place: (0,) * array.ndim)
    step_block = pl.BlockSpec((frames, 2 * width), lambda s, cols, place: (0, s))
    return call(
        partial(own_terms_body, len(ups), spots_of_sum(ups, width)),
        grid_spec=pltpu.PrefetchScalarGridSpec(
            num_scalar_prefetch=2,
            grid=(2,),
            in_specs=[whole(grad)]
            + [part_spec(up, frames) for up in ups]
            + weight_specs(weights, layer),
            out_specs=step_block,
            scratch_shapes=[pltpu.VMEM((4, frames, width), BF16)] * 2 + [far_scratch(weights)],
        ),
        out_shape=jax.ShapeDtypeStruct((frames, features), F32),
        cost_estimate=cost(6 * frames * features * features, 4 * features * features),
        name="own_terms",
    )(columns, place, in_hbm(grad), *arrays_of(ups), *[in_hbm(w) for w in weights])


def prepare_body(n_chunks, lists_ref, place_ref, *refs):
    del lists_ref
    groups = []
    for _ in range(4):
        groups.append(refs[:n_chunks])
        refs = refs[n_chunks:]
    high_ref, low_ref = refs
    padded = high_ref.shape[0] // 2
    width = high_ref.shape[1] // 2
    for side in range(2):

        @pl.when(pl.program_id(0) // 2 == side)
        def _():
            for clip in range(2):
                for dc in range(2):
                    at = pl.multiple_of((place_ref[6] ^ clip ^ dc) * width, width)
                    row = clip * padded
                    for part in groups[2 * clip + side]:
                        rows = part.shape[0]
                        high, low = split(part[:, dc * width : (dc + 1) * width])
                        high_ref[row : row + rows, pl.ds(at, width)] = high
                        low_ref[row : row + rows, pl.ds(at, width)] = low
                        row += rows
                rest = (clip + 1) * padded - row
                zeros = jnp.zeros((rest, 2 * width), BF16)
                high_ref[row : row + rest, :] = zeros
                low_ref[row : row + rest, :] = zeros


def prepare(lists, place, groups):
    width = groups[0][0].shape[1] // 4
    frames = sum(part.shape[0] for part in groups[0])
    padded = -(-frames // LANES) * LANES
    in_specs = []
    for i, group in enumerate(groups):
        for part in group:
            if i % 2 == 0:
                index = lambda s, *_: (0, jnp.minimum(s, 1))
            else:
                index = lambda s, *_: (0, jnp.maximum(s - 2, 0))
            in_specs.append(pl.BlockSpec((part.shape[0], 2 * width), index))
    out = jax.ShapeDtypeStruct((2 * padded, 8 * width), BF16)
    out_spec = pl.BlockSpec((2 * padded, 2 * width), lambda s, cols, place: (0, cols[s]))
    return call(
        partial(prepare_body, len(groups[0])),
        grid_spec=pltpu.PrefetchScalarGridSpec(
            num_scalar_prefetch=2,
            grid=(4,),
            in_specs=in_specs,
            out_specs=[out_spec, out_spec],
        ),
        out_shape=[out, out],
        hbm_outs=(0, 1),
        cost_estimate=cost(0, 16 * frames * 8 * width),
        name="prepare",
    )(lists, place, *[in_hbm(part) for group in groups for part in group])


def product(g_high, g_low, x_high, x_low):
    return dot(g_high, x_high, NN) + (dot(g_high, x_low, NN) + dot(g_low, x_high, NN))


def weight_body(turn, place_ref, *refs):
    if turn:
        grad_ref, near_ref, x_high, x_low, kept, sent, g_high, g_low, t_high, t_low = refs

        @pl.when(pl.program_id(0) == 0)
        def _():
            frames, features = grad_ref.shape
            width = features // 4
            rows = width // 4
            padded = t_high.shape[1] // 2
            t_high[...] = jnp.zeros_like(t_high)
            t_low[...] = jnp.zeros_like(t_low)
            for clip in range(2):
                for dh in range(2):
                    if clip == 0:
                        part = grad_ref[:, 2 * dh * width : (2 * dh + 1) * width]
                    else:
                        part = near_ref[:, dh * width : (dh + 1) * width]
                    high, low = split(part.T)
                    at = (
                        slice(dh * width, (dh + 1) * width),
                        slice(clip * padded, clip * padded + frames),
                    )
                    t_high[at] = high
                    t_low[at] = low
            for group in range(8):
                first, second, dh = group // 4, group // 2 % 2, group % 2
                core = place_ref[6]
                y = place_ref[4] ^ (first * core + second * (1 - core))
                x = place_ref[5] ^ (first * (1 - core) + second * core)
                at = pl.multiple_of(dh * width + (2 * y + x) * rows, rows)
                g_high[group * rows : (group + 1) * rows, :] = t_high[pl.ds(at, rows), :]
                g_low[group * rows : (group + 1) * rows, :] = t_low[pl.ds(at, rows), :]

    else:
        g_high, g_low, x_high, x_low, kept, sent = refs
    half = g_high.shape[0] // 2
    value = product(g_high[...], g_low[...], x_high[...], x_low[...])
    kept[...] = value[:half].reshape(kept.shape)
    sent[...] = value[half:].reshape(sent.shape)


def weight_rows(half, place, grads, x_split, width):
    turn = half == 0
    whole = lambda array: pl.BlockSpec(array.shape, lambda s, place: (0,) * array.ndim)
    x_spec = pl.BlockSpec((x_split[0].shape[0], width), lambda s, place: (0, 4 * half + s))
    shape = (2, 2, width // 4, 4 * width)
    out_shape = [jax.ShapeDtypeStruct(shape, F32)] * 2
    out_specs = [pl.BlockSpec(shape[:3] + (width,), lambda s, place: (0, 0, 0, s))] * 2
    scratch = []
    if turn:
        turned = (2 * width, x_split[0].shape[0])
        out_shape += [jax.ShapeDtypeStruct(turned, BF16)] * 2
        out_specs += [whole(out_shape[-1])] * 2
        scratch = [pltpu.VMEM(turned, BF16)] * 2
    return call(
        partial(weight_body, turn),
        grid_spec=pltpu.PrefetchScalarGridSpec(
            num_scalar_prefetch=1,
            grid=(4,),
            in_specs=[whole(a) for a in grads] + [x_spec] * 2,
            out_specs=out_specs,
            scratch_shapes=scratch,
        ),
        out_shape=out_shape,
        hbm_outs=(0,),
        cost_estimate=cost(12 * x_split[0].shape[0] * width * 4 * width, 4 * 8 * width * width),
        name="weight_rows",
    )(place, *([in_hbm(grads[0]), grads[1]] if turn else grads), *[in_hbm(x) for x in x_split])


def step_body(n, widths, cut, *refs):
    ins, outs = refs[: 2 * n], refs[2 * n :]
    starts = [sum(widths[:i]) for i in range(len(widths))]
    column = 0
    for i in range(n):
        total = ins[2 * i][...] + ins[2 * i + 1][...]
        end = column + total.shape[-1]
        for j, (start, columns) in enumerate(zip(starts, widths)):
            low, high = max(start, column), min(start + columns, end)
            if low < high:
                to = (Ellipsis, slice(low - start, high - start))
                piece = total[..., low - column : high - column]
                if cut:
                    outs[2 * j][to] = piece[0]
                    outs[2 * j + 1][to] = piece[1]
                else:
                    outs[j][to] = piece
        column = end


def step_of(*pairs, cut=True, widths=None):
    shape = list(pairs[0][0].shape)
    widths = widths or [sum(pair[0].shape[-1] for pair in pairs)]
    outs = []
    for columns in widths:
        shape[-1] = columns
        out = jax.ShapeDtypeStruct(tuple(shape[1:] if cut else shape), F32)
        outs += [out] * (1 + cut)
    whole = lambda array: pl.BlockSpec(array.shape, lambda i: (0,) * array.ndim)
    operands = [array for pair in pairs for array in pair]
    return call(
        partial(step_body, len(pairs), widths, cut),
        grid=(1,),
        in_specs=[whole(a) for a in operands],
        out_specs=[whole(a) for a in outs],
        out_shape=outs,
        cost_estimate=cost(0, 4 * sum(a.size for a in operands)),
        name="reduction_step",
    )(*operands)


def plane_swap(array, step):
    pairs = []
    for i in range(8):
        over_x = (i % 2 == 0) == (step == 0)
        pairs.append((i, i ^ 2 if over_x else i ^ 4))
    return lax.ppermute(array, ("y", "x", "c"), pairs)


def plane_gather(share, *before):
    first = plane_swap(share, 0)
    second = plane_swap(share, 1)
    return [share, second, first, plane_swap(after(first, *before), 1)]


def assemble_body(groups, place_ref, *refs):
    out_ref = refs[-1]
    core = place_ref[6]
    column = 0
    for group in range(groups):
        rows, columns = refs[4 * group].shape
        for i in range(4):
            first, second = i // 2, i % 2
            y = place_ref[4] ^ (first * core + second * (1 - core))
            x = place_ref[5] ^ (first * (1 - core) + second * core)
            at = pl.multiple_of((2 * y + x) * rows, rows)
            out_ref[0, pl.ds(at, rows), column : column + columns] = refs[4 * group + i][...]
        column += columns


def assemble(place, groups, layer, onto=None):
    pieces = [piece for group in groups for piece in group]
    rows = 4 * pieces[0].shape[0]
    columns = sum(group[0].shape[1] for group in groups)
    aliases, extra, extra_specs = {}, [], []
    if onto is not None:
        aliases, extra = {1 + len(pieces): 0}, [onto]
        extra_specs = [pl.BlockSpec(memory_space=pl.ANY)]
    (out,) = call(
        partial(assemble_body, len(groups)),
        grid=(1,),
        out_shape=[jax.ShapeDtypeStruct((LAYERS, rows, columns), F32)],
        hbm_outs=(0,),
        in_specs=[SMEM_SPEC]
        + [pl.BlockSpec(p.shape, lambda i: (0, 0)) for p in pieces]
        + extra_specs,
        out_specs=[pl.BlockSpec((1, rows, columns), lambda i: (layer, 0, 0))],
        input_output_aliases=aliases,
        cost_estimate=cost(0, 8 * rows * columns),
        name="assemble",
    )(place, *[p if extra else in_hbm(p) for p in pieces], *extra)
    return out


def half_features(inputs, weights, gains, shifts, decays, biases, lengths, frame_mask, grad_out):
    width, slots = inputs.shape
    clips, frames = frame_mask.shape
    depth = weights.shape[2]
    blocks = 4 * width // LANES
    y, x, h, l, c = (lax.axis_index(name) for name in ("y", "x", "h", "l", "c"))
    b = 2 * y + x
    numbers = [2 * (h ^ (rel // 2)) + (c ^ (rel % 2)) for rel in range(4)] + [y, x, c]
    place = jnp.stack(numbers).astype(jnp.int32)
    own_blocks, other_blocks = (
        jnp.stack(
            [2 * (2 * (h ^ (rel // 2)) + half) + (c ^ (rel % 2)) for rel in range(4)]
        ).astype(jnp.int32)
        for half in (l, 1 - l)
    )
    own_columns = jnp.stack([2 * h + l, 2 * (1 - h) + l]).astype(jnp.int32)
    other_columns = jnp.stack([2 * (1 - h) + 1 - l, 2 * h + 1 - l]).astype(jnp.int32)
    all_columns = jnp.concatenate([own_columns, other_columns[::-1]])
    rows = width // 4

    clip = 2 * h + c
    seen = lax.dynamic_index_in_dim(frame_mask, clip, 0, keepdims=False)
    length = lax.dynamic_index_in_dim(lengths, clip, 0, keepdims=False)
    moments = jnp.arange(frames, dtype=jnp.int32)
    gate = ((moments < length) & ((seen == 1) | (moments == 0))).astype(F32)
    valid = jnp.broadcast_to(gate[:, None], (frames, LANES))

    def far_share(layer):
        return lax.dynamic_slice(weights, (layer, b * rows, 0), (1, rows, depth))[0]

    def over_h(array):
        return lax.ppermute(array, "h", FLIP2)

    def over_c(array):
        return lax.ppermute(array, "c", FLIP2)

    def over_second(array):
        return plane_swap(array, 1)

    def four_of(near_rows, far_rows):
        return [
            (near_rows, 0),
            (over_c(near_rows), 1),
            (far_rows, 0),
            (over_c(far_rows), 1),
        ]

    def far_pieces(share):
        both = lax.ppermute(share, ("y", "x"), DIAGONAL)
        return [share, lax.ppermute(share, "x", FLIP2), lax.ppermute(share, "y", FLIP2), both]

    near = over_c(weights)
    share = far_share(0)
    close, away = pack(place, after(inputs, share), frames)
    share = over_h(share)
    away = over_h(away)
    other_close = swap_half(close)
    up_close, up_away = pack(place, after(grad_out, close), frames, waits=True)
    share = after(share, up_close, valid, near, other_close)
    pieces = far_pieces(share)
    away = after(away, pieces[1:])
    half_weights = [[weights, near, *pieces, *map(over_c, after(pieces, away))]]
    own = four_of(after(close, away), away)
    other_away = swap_half(away)
    params = jnp.stack([gains, shifts + biases, decays], axis=1)
    own_params = params.reshape(LAYERS * 3 * width // LANES, LANES)
    params = None

    saved = []
    for layer in range(LAYERS):
        last = layer == LAYERS - 1
        flat = layer == 0
        if layer > 0:
            others = [(swap_half(array), None) for array, _ in own]
        z, *own_flat = project(
            own_blocks, place, frames, own, half_weights[layer], layer, flat=flat
        )
        if flat:
            others = four_of(other_close, after(other_away, z))
        z, stats, *other_flat = project(
            other_blocks,
            place,
            frames,
            others,
            half_weights[layer],
            layer,
            z,
            valid,
            own_params if flat else None,
            flat,
        )
        if last:
            upstream = four_of(up_close, after(up_away, z))
        if flat:
            stats = lax.all_gather(stats, ("h", "c"), tiled=True)
            share = over_h(after(far_share(1), stats))
            stats = lax.all_gather(stats, ("y", "x"), tiled=True)
        else:
            stats = lax.all_gather(stats, ("y", "x"), tiled=True)
            stats = lax.all_gather(stats, ("h", "c"), tiled=True)
        if flat:
            own = [(own_flat[0], None)]
        *following, states, slopes = recur(
            layer, place, gate, z, stats, params, valid, own, last
        )
        if flat:
            *following, states, slopes, params = *following, states, slopes
            groups = [own_flat, other_flat]
        else:
            groups = [arrays_of(own), arrays_of(others)]
        groups += [[over_c(after(p, z)) for p in group] for group in groups]
        x_split = prepare(all_columns, place, after(groups, slopes)) if flat else None
        if flat:
            up_away = over_h(after(up_away, x_split[0]))
            pieces = far_pieces(after(share, slopes))
            half_weights.append([weights, near, *pieces, *map(over_c, pieces)])
        saved.append((groups, x_split, z, stats, states, slopes))
        own = [(array, None) for array in following]
    output, away, diagonal = following
    diagonal = over_c(over_h(diagonal))

    ups = upstream
    results = [None] * LAYERS
    for layer in range(LAYERS - 1, -1, -1):
        groups, x_split, z, stats, states, slopes = saved[layer]
        weight = half_weights[layer]
        grad_pre, sums = back(
            layer, place, gate, z, stats, params, ups, [states], [slopes]
        )
        plane = lax.all_gather(sums, ("y", "x"), tiled=True)
        if layer == 0:
            later, go = step_of(*[(in_hbm(k), after(g, plane)) for k, g in zip(stay, come)])
            plane = after(plane, later)
            go = over_second(go)
        sums = lax.all_gather(plane, ("h", "c"), tiled=True)
        if layer > 0:
            away = over_h(after(away, sums))
        grad_z, leaving, *terms, sums = norm_back(
            other_columns, place, grad_pre, z, params, valid, stats, sums, weight, layer,
            layer == 0,
        )
        leaving = over_c(leaving)
        if layer > 0:
            received = [swap_half(terms[0])]
            x_split = prepare(all_columns, place, after(groups, grad_z, diagonal))
        else:
            received = [None, swap_half(terms[1])]
            later, go = step_of((later, after(go, grad_z)))
            leaving = after(leaving, later)
            later = (later, over_h(go))
        *first, g_high, g_low = weight_rows(0, place, (grad_z, leaving), x_split, width)
        turned = (g_high, g_low)
        come = [plane_swap(first[1], 0)]
        if layer > 0:
            turned = after(turned, away)
            output = [(output, 0), (over_c(output), 1), (away, 0), (diagonal, 0)]
        else:
            received[0] = swap_half(after(terms[0], received[1]))
        second = weight_rows(1, place, turned, x_split, width)
        come.append(plane_swap(second[1], 0))
        stay = (first[0], second[0])
        kept = own_terms(own_columns, place, after(grad_z, second[0]), ups, weight, layer)
        ups = [(kept, None)] + [(r, None) for r in received]
        results[layer] = lax.dynamic_index_in_dim(
            sums.reshape(3, 4, width), clip, axis=1, keepdims=False
        )

    away = merge(kept, 1, received[1])
    (later,) = step_of((later[0], after(later[1], away)), cut=False)
    away = over_h(away)
    later_first, later_second = plane_swap(later, 0), plane_swap(later, 1)
    total, go = step_of((in_hbm(stay[0]), after(come[0], later_first)), (in_hbm(stay[1]), come[1]))
    go = over_second(go)
    later = [later, later_second, later_first, plane_swap(after(later_first, total), 1)]
    far = [(away, 0), (over_c(away), 1)]
    grad_weights = assemble(place, [later], 1)
    halves = step_of((total, after(go, far[1][0], grad_weights)), widths=[depth // 2] * 2)
    first, second = (halves[0], over_h(halves[1])), (halves[2], over_h(halves[3]))
    output = unpack(
        place, [(after(array, first[0]), i) for array, i in output], frames, waited=True
    )
    close = merge(kept, 0, after(received[0], output))
    grad_in = [(close, 0), (over_c(close[frames:]), 0)] + far
    (first,) = step_of((first[0], after(first[1], close)), cut=False)
    gathered = [plane_gather(first)]
    (second,) = step_of((second[0], after(second[1], gathered[0][2])), cut=False)
    gathered.append(plane_gather(second))
    grad_in = unpack(place, [(after(array, second), i) for array, i in grad_in], frames)
    grad_weights = assemble(place, after(gathered, grad_in), 0, grad_weights)
    sums = jnp.stack(results)
    return (
        output,
        grad_in,
        grad_weights,
        sums[:, 0],
        sums[:, 1],
        sums[:, 2],
        sums[:, 1],
    )


def gelu_slope(value):
    return (
        0.5 * (1.0 + jax.scipy.special.erf(value / ROOT_TWO))
        + value * jnp.exp(-0.5 * value * value) / ROOT_TWO_PI
    )


def recur_step(decay, state, inputs):
    drive_t, valid_t = inputs
    pre = drive_t + decay * state
    state = state + valid_t * (jax.nn.gelu(pre, approximate=False) - state)
    return (state, state)


def back_step(decay, carry, inputs):
    upstream_t, valid_t, pre_t = inputs
    total = upstream_t + carry
    grad_pre = total * valid_t * gelu_slope(pre_t)
    carry = total * (1.0 - valid_t) + grad_pre * decay
    return (carry, grad_pre)


def add_piece(weight, piece):
    return jnp.dot(weight, piece, precision=HIGH, preferred_element_type=jnp.float32)


def weight_columns(grad_pre_norm, piece):
    return jnp.einsum("jf,kf->jk", grad_pre_norm, piece, precision=HIGH)


def split_features(inputs, weights, gains, shifts, decays, biases, lengths, frame_mask, grad_out):
    width, slots = inputs.shape
    clips, frames_len = frame_mask.shape
    frames = jnp.arange(frames_len, dtype=jnp.int32)
    valid_grid = (
        (frames[None, :] < lengths[:, None]) & ((frame_mask == 1) | (frames[None, :] == 0))
    ).astype(jnp.float32)
    valid = valid_grid.reshape(-1)
    valid_row = valid[None, :]
    valid_time = jnp.broadcast_to(valid_grid.T[:, :, None], (frames_len, clips, width)).reshape(
        frames_len, clips * width
    )
    count_local = jnp.sum(valid)

    def to_time(array):
        return jnp.transpose(array.reshape(width, clips, frames_len), (2, 1, 0)).reshape(
            frames_len, clips * width
        )

    def from_time(array):
        return jnp.transpose(array.reshape(frames_len, clips, width), (2, 1, 0)).reshape(
            width, slots
        )

    layer_in = inputs
    saved = []
    for layer_no in range(LAYERS):
        weight = weights[layer_no]
        gathered = lax.all_gather(layer_in, "neuron", axis=0, tiled=True)
        pre_norm = add_piece(weight, gathered)
        first_sum, count = lax.psum((jnp.sum(valid_row * pre_norm, axis=1), count_local), "batch")
        mean = first_sum / count
        centered = pre_norm - mean[:, None]
        var = lax.psum(jnp.sum(valid_row * centered * centered, axis=1), "batch") / count
        inv_std = lax.rsqrt(var + EPS)
        zhat = (pre_norm - mean[:, None]) * inv_std[:, None]
        drive = gains[layer_no][:, None] * zhat + (shifts[layer_no] + biases[layer_no])[:, None]
        drive_time = to_time(drive)
        decay_wide = jnp.tile(decays[layer_no], clips)
        start_state = jnp.zeros((clips * width,), jnp.float32)
        _, states = lax.scan(
            partial(recur_step, decay_wide), start_state, (drive_time, valid_time), unroll=8
        )
        saved.append((gathered, zhat, inv_std, drive_time, states, count))
        layer_in = layer_in + valid_row * from_time(states)
    upstream = grad_out
    grad_parts = [None] * LAYERS
    for layer_no in range(LAYERS - 1, -1, -1):
        gathered, zhat, inv_std, drive_time, states, count = saved[layer_no]
        decay_wide = jnp.tile(decays[layer_no], clips)
        gain = gains[layer_no]
        previous = jnp.concatenate([jnp.zeros_like(states[:1]), states[:-1]], axis=0)
        pre_time = drive_time + decay_wide[None, :] * previous
        grad_state = to_time(valid_row * upstream)
        start_carry = jnp.zeros((clips * width,), jnp.float32)
        _, grad_pre_time = lax.scan(
            partial(back_step, decay_wide),
            start_carry,
            (grad_state, valid_time, pre_time),
            reverse=True,
            unroll=8,
        )
        decay_local = jnp.sum(
            jnp.sum(grad_pre_time * previous, axis=0).reshape(clips, width), axis=0
        )
        grad_pre = from_time(grad_pre_time)
        gain_local = jnp.sum(grad_pre * zhat, axis=1)
        shift_local = jnp.sum(grad_pre, axis=1)
        grad_gain, grad_shift, grad_decay = lax.psum(
            (gain_local, shift_local, decay_local), "batch"
        )
        grad_pre_norm = (gain * inv_std)[:, None] * (
            grad_pre - valid_row * (grad_shift[:, None] + zhat * grad_gain[:, None]) / count
        )
        weight_local = weight_columns(grad_pre_norm, gathered)
        input_terms = jnp.einsum("jk,jf->kf", weights[layer_no], grad_pre_norm, precision=HIGH)
        input_grad = lax.psum_scatter(input_terms, "neuron", scatter_dimension=0, tiled=True)
        grad_weight = lax.psum(weight_local, "batch")
        upstream = upstream + input_grad
        grad_parts[layer_no] = (grad_weight, grad_gain, grad_shift, grad_decay)
    grad_weights = jnp.stack([grad_parts[layer_no][0] for layer_no in range(LAYERS)])
    grad_gains = jnp.stack([grad_parts[layer_no][1] for layer_no in range(LAYERS)])
    grad_shifts = jnp.stack([grad_parts[layer_no][2] for layer_no in range(LAYERS)])
    grad_decays = jnp.stack([grad_parts[layer_no][3] for layer_no in range(LAYERS)])
    return (layer_in, upstream, grad_weights, grad_gains, grad_shifts, grad_decays, grad_shifts)


def solution(mesh):
    if (mesh.shape["batch"], mesh.shape["neuron"]) == (4, 8):
        cut = Mesh(mesh.devices.reshape(2, 2, 2, 2, 2), ("y", "x", "h", "l", "c"))
        batch, neuron, body = ("y", "x"), ("h", "l", "c"), half_features
    else:
        cut, batch, neuron, body = mesh, "batch", "neuron", split_features
    in_specs = (
        P(neuron, batch),
        P(None, neuron, None),
        P(None, neuron),
        P(None, neuron),
        P(None, neuron),
        P(None, neuron),
        P(batch),
        P(batch, None),
        P(neuron, batch),
    )
    out_specs = (
        P(neuron, batch),
        P(neuron, batch),
        P(None, neuron, None),
        P(None, neuron),
        P(None, neuron),
        P(None, neuron),
        P(None, neuron),
    )
    return jax.shard_map(
        body, mesh=cut, in_specs=in_specs, out_specs=out_specs, check_vma=False
    )
```

```python
from functools import partial
import math

import jax
import jax.numpy as jnp
from jax import lax
from jax.experimental import pallas as pl
from jax.experimental.pallas import tpu as pltpu
from jax.sharding import Mesh, PartitionSpec as P

LAYERS = 2
EPS = 1e-05
HIGH = lax.Precision.HIGHEST
ROOT_TWO = math.sqrt(2.0)
ROOT_TWO_PI = math.sqrt(2.0 * math.pi)
F32 = jnp.float32
BF16 = jnp.bfloat16
LANES = 128
VMEM_LIMIT = 24 * 1024 * 1024
SMEM_SPEC = pl.BlockSpec(memory_space=pltpu.SMEM)
VMEM_SPEC = pl.BlockSpec(memory_space=pltpu.VMEM)


FLIP2 = [(0, 1), (1, 0)]
DIAGONAL = [(0, 3), (1, 2), (2, 1), (3, 0)]


def swap_half(array):
    return lax.ppermute(array, "l", FLIP2)


def after(value, *others):
    return lax.optimization_barrier((value, others))[0]


def split(value):
    high = value.astype(BF16)
    return high, (value - high.astype(F32)).astype(BF16)


def dot(a, b, dims):
    return lax.dot_general(a, b, (dims, ((), ())), preferred_element_type=F32)


NT = ((1,), (1,))
NN = ((1,), (0,))


def in_hbm(array):
    return pltpu.with_memory_space_constraint(array, pltpu.HBM)


def call(body, out_shape, hbm_outs=(), **kwargs):
    if hbm_outs:
        out_shape = [
            pltpu.HBM(a.shape, a.dtype) if i in hbm_outs else a for i, a in enumerate(out_shape)
        ]
    return pl.pallas_call(
        body,
        out_shape=out_shape,
        compiler_params=pltpu.CompilerParams(vmem_limit_bytes=VMEM_LIMIT),
        **kwargs,
    )


def cost(flops, byte_count):
    return pl.CostEstimate(flops=int(flops) // 64, bytes_accessed=int(byte_count) // 64, transcendentals=0)


def pack_body(frames, place_ref, in_ref, near_ref, far_ref, turned):
    slots = in_ref.shape[1]
    for start in range(0, slots, LANES):
        turned[start : start + LANES, :] = in_ref[:, start : start + LANES].T
    for rel in range(4):
        first = pl.multiple_of(place_ref[rel] * frames, 8)
        out = (near_ref, far_ref)[rel // 2]
        out[(rel % 2) * frames : (rel % 2 + 1) * frames, :] = turned[pl.ds(first, frames), :]


def pack(place, array, frames, waits=False):
    width, slots = array.shape
    out = jax.ShapeDtypeStruct((2 * frames, width), F32)
    return call(
        partial(pack_body, frames),
        grid=(1,),
        out_shape=[out, out],
        in_specs=[SMEM_SPEC, pl.BlockSpec((width, slots), lambda i: (0, 0))],
        out_specs=[pl.BlockSpec(out.shape, lambda i: (0, 0))] * 2,
        scratch_shapes=[pltpu.VMEM((slots, width), F32)],
        hbm_outs=(0, 1) if waits else (),
        cost_estimate=cost(0, 8 * width * slots),
        name="pack",
    )(place, in_hbm(array))


def part_spec(part, frames):
    array, i = part
    if i is None:
        return pl.BlockSpec(array.shape, lambda *_: (0,) * array.ndim)
    return pl.BlockSpec((frames, array.shape[1]), lambda *_: (i, 0))


def arrays_of(parts):
    return [array for array, _ in parts]


def unpack_body(frames, place_ref, *refs):
    ins, out_ref, turned = refs[:4], refs[4], refs[5]
    slots = out_ref.shape[1]
    for rel in range(4):
        first = pl.multiple_of(place_ref[rel] * frames, 8)
        turned[pl.ds(first, frames), :] = ins[rel][...]
    for start in range(0, slots, LANES):
        out_ref[:, start : start + LANES] = turned[start : start + LANES, :].T


def unpack(place, parts, frames, waited=False):
    width = parts[0][0].shape[1]
    slots = 4 * frames
    return call(
        partial(unpack_body, frames),
        grid=(1,),
        out_shape=jax.ShapeDtypeStruct((width, slots), F32),
        in_specs=[SMEM_SPEC] + [part_spec(part, frames) for part in parts],
        out_specs=pl.BlockSpec((width, slots), lambda i: (0, 0)),
        scratch_shapes=[pltpu.VMEM((slots, width), F32)],
        cost_estimate=cost(0, 8 * width * slots),
        name="unpack",
    )(place, *[in_hbm(a) if waited else a for a in arrays_of(parts)])


def merge_body(kept_ref, come_ref, out_ref):
    frames, columns = kept_ref.shape
    width = columns // 2
    for i in range(2):
        some = slice(i * width, (i + 1) * width)
        out_ref[i * frames : (i + 1) * frames, :] = kept_ref[:, some] + come_ref[:, some]


def merge(kept, half, come):
    frames, columns = come.shape
    return call(
        merge_body,
        grid=(1,),
        out_shape=jax.ShapeDtypeStruct((2 * frames, columns // 2), F32),
        in_specs=[
            pl.BlockSpec((frames, columns), lambda i: (0, half)),
            pl.BlockSpec((frames, columns), lambda i: (0, 0)),
        ],
        out_specs=pl.BlockSpec((2 * frames, columns // 2), lambda i: (0, 0)),
        cost_estimate=cost(0, 12 * frames * columns),
        name="merge",
    )(kept, come)


def spread_of(parts, width):
    spots, row, column = [], 0, 0
    for array, _ in parts:
        spots.append((row, column))
        if array.shape[1] == width:
            column += width
        else:
            row += array.shape[0]
    return spots


def project_body(n_parts, spots, with_acc, with_stats, with_params, flat, cols_ref, place_ref, *refs):
    del cols_ref
    parts, refs = refs[:n_parts], refs[n_parts:]
    weights, refs = refs[:10], refs[10:]
    if with_acc:
        acc_ref, refs = refs[0], refs[1:]
    if with_stats:
        valid_ref, refs = refs[0], refs[1:]
    if with_params:
        params_ref, refs = refs[0], refs[1:]
    out_ref, refs = refs[0], refs[1:]
    if with_stats:
        stats_ref, refs = refs[0], refs[1:]
    if flat:
        flat_ref, refs = refs[0], refs[1:]
    x_high, x_low, far_ref = refs
    step = pl.program_id(0)
    width = x_high.shape[2]

    @pl.when(step == 0)
    def _():
        for (row, column), part in zip(spots, parts):
            rows, columns = part.shape
            for start in range(0, columns, width):
                rel = (column + start) // width
                high, low = split(part[:, start : start + width])
                x_high[rel, row : row + rows, :] = high
                x_low[rel, row : row + rows, :] = low
            if flat:
                flat_ref[row : row + rows, column : column + columns] = part[...]
        if with_acc:
            out_ref[...] = acc_ref[...]
        else:
            out_ref[...] = jnp.zeros_like(out_ref)

    stacked = jnp.concatenate([x_high[step], x_low[step], x_high[step]], axis=1)
    for block, weight in enumerate(weight_blocks(place_ref, weights, far_ref)):
        w_high, w_low = split(weight)
        columns = slice(block * width, (block + 1) * width)
        out_ref[:, columns] += dot(stacked, jnp.concatenate([w_high, w_high, w_low], axis=1), NT)

    if with_stats:

        @pl.when(step == pl.num_programs(0) - 1)
        def _():
            valid = valid_ref[...]
            own = jnp.sum(valid, axis=0, keepdims=True)
            per = width // LANES
            for row in range(out_ref.shape[1] // LANES):
                z = out_ref[:, row * LANES : (row + 1) * LANES]
                total = jnp.sum(valid * z, axis=0, keepdims=True)
                centred = valid * (z - total / own)
                squares = jnp.sum(centred * centred, axis=0, keepdims=True)
                at = place_ref[row // per] * per + row % per
                stats_ref[0, pl.ds(at, 1), :] = total
                stats_ref[1, pl.ds(at, 1), :] = squares
                stats_ref[2, pl.ds(at, 1), :] = own
            if with_params:
                rest = params_ref.shape[0] - 8
                stats_ref[3] = params_ref[:8, :]
                stats_ref[4] = jnp.zeros_like(stats_ref[4])
                stats_ref[4, :rest, :] = params_ref[8:, :]


def weight_specs(weights, layer, pairs=2):
    width = weights[0].shape[1]
    specs = []
    for weight in weights:
        if weight.ndim == 3:
            specs.append(
                pl.BlockSpec((1, width, pairs * width), lambda s, cols, *_: (layer, 0, cols[s]))
            )
        else:
            rows = weight.shape[0]
            specs.append(pl.BlockSpec((rows, pairs * width), lambda s, cols, *_: (0, cols[s])))
    return specs


def far_scratch(weights, pairs=2):
    width = weights[0].shape[1]
    return pltpu.VMEM((2, width, pairs * width), F32)


def weight_blocks(place_ref, refs, far_ref):
    for i in range(2):
        for rel, piece in enumerate(refs[2 + 4 * i : 6 + 4 * i]):
            rows = piece.shape[0]
            row = 2 * (place_ref[4] ^ (rel // 2)) + (place_ref[5] ^ (rel % 2))
            far_ref[i, pl.ds(pl.multiple_of(row * rows, rows), rows), :] = piece[...]
    return [refs[0][0], refs[1][0], far_ref[0], far_ref[1]]


def project(
    columns, place, frames, parts, weights, layer, acc=None, valid=None, params=None, flat=False
):
    width = weights[0].shape[-2]
    full = pl.BlockSpec(memory_space=pltpu.VMEM)
    in_specs = [part_spec(part, frames) for part in parts]
    in_specs += weight_specs(weights, layer, 1)
    operands = arrays_of(parts) + [in_hbm(w) for w in weights]
    array = jax.ShapeDtypeStruct((frames, 4 * width), F32)
    array_spec = pl.BlockSpec((frames, 4 * width), lambda s, cols, place: (0, 0))
    out_shape, out_specs = [array], [array_spec]
    if acc is not None:
        in_specs.append(array_spec)
        operands.append(in_hbm(acc))
    if valid is not None:
        in_specs.append(full)
        operands.append(valid)
        stats = (3 if params is None else 5, 4 * width // LANES, LANES)
        out_shape.append(jax.ShapeDtypeStruct(stats, F32))
        out_specs.append(pl.BlockSpec(stats, lambda s, cols, place: (0, 0, 0)))
    if params is not None:
        in_specs.append(full)
        operands.append(params)
    if flat:
        out_shape.append(array)
        out_specs.append(array_spec)
    return call(
        partial(
            project_body,
            len(parts),
            spread_of(parts, width),
            acc is not None,
            valid is not None,
            params is not None,
            flat,
        ),
        grid_spec=pltpu.PrefetchScalarGridSpec(
            num_scalar_prefetch=2,
            grid=(4,),
            in_specs=in_specs,
            out_specs=out_specs,
            scratch_shapes=[pltpu.VMEM((4, frames, width), BF16)] * 2 + [far_scratch(weights, 1)],
        ),
        out_shape=out_shape,
        hbm_outs=(0, len(out_shape) - 1) if flat else (0,),
        cost_estimate=cost(2 * 3 * frames * 16 * width * width, 4 * 16 * width * width),
        name="project",
    )(columns, place, *operands)


def to_relative(place_ref, spread, rows_ref, value, slot):
    per = value.shape[0] // 4
    spread[...] = value
    for rel in range(4):
        first = place_ref[rel] * per
        for row in range(per):
            rows_ref[slot, rel * per + row : rel * per + row + 1, :] = spread[
                pl.ds(first + row, 1), :
            ]


def tree(values):
    while len(values) > 1:
        values = [a + b for a, b in zip(values[::2], values[1::2])]
    return values[0]


def norm_terms(stats_ref):
    step = stats_ref.shape[0] // 16
    each = [[stats_ref[i] for i in range(slot, stats_ref.shape[0], step)] for slot in range(3)]
    totals, squares, owns = each
    count = tree(owns)
    mean = tree(totals) / count
    away = [total / own - mean for total, own in zip(totals, owns)]
    spread = tree([s + n * a * a for s, n, a in zip(squares, owns, away)])
    return count, mean, lax.rsqrt(spread / count + EPS)


def recur_body(n_parts, spots, last, layer, spread_params, place_ref, gate_ref, z_ref, stats_ref, params_ref, valid_ref, *refs):
    parts, refs = refs[:n_parts], refs[n_parts:]
    outs, refs = refs[: 1 + 2 * last], refs[1 + 2 * last :]
    if spread_params:
        state_ref, slope_ref, params_out, rows, spread, drive_s, state_s, slope_s = refs
    else:
        state_ref, slope_ref, rows, spread, drive_s, state_s, slope_s = refs
    frames = z_ref.shape[0]
    blocks = z_ref.shape[1] // LANES
    per = blocks // 4
    if spread_params:
        for rel in range(4):
            first = place_ref[rel] * (stats_ref.shape[0] // 16)
            for row in range(LAYERS * 3 * per):
                params_out[row // per, rel * per + row % per : rel * per + row % per + 1, :] = (
                    stats_ref[first + 3 + row // 8, row % 8 : row % 8 + 1, :]
                )
        params = [params_out[3 * layer + i] for i in range(3)]
    else:
        params = [params_ref[3 * layer + i] for i in range(3)]
    _, mean, inv_std = norm_terms(stats_ref)
    to_relative(place_ref, spread, rows, mean, 0)
    to_relative(place_ref, spread, rows, inv_std, 1)
    rows[1] = rows[1] * params[0]
    rows[2] = params[1]
    decay = params[2]
    for row in range(blocks):
        z = z_ref[:, row * LANES : (row + 1) * LANES]
        drive_s[row * frames : (row + 1) * frames, :] = (
            z - rows[0, row : row + 1, :]
        ) * rows[1, row : row + 1, :] + rows[2, row : row + 1, :]

    def step(t, state):
        at = pl.ds(t, blocks, stride=frames)
        pre = drive_s[at, :] + decay * state
        half = 0.5 + 0.5 * lax.erf(pre * (1.0 / ROOT_TWO))
        gate = gate_ref[t] > 0.0
        slope = half + pre * jnp.exp(-0.5 * pre * pre) * (1.0 / ROOT_TWO_PI)
        state = jnp.where(gate, pre * half, state)
        state_s[at, :] = state
        slope_s[at, :] = jnp.where(gate, slope, 0.0)
        return state

    lax.fori_loop(0, frames, step, jnp.zeros((blocks, LANES), F32), unroll=8)
    valid = valid_ref[...]
    for row in range(blocks):
        lanes = slice(row * LANES, (row + 1) * LANES)
        state = state_s[row * frames : (row + 1) * frames, :]
        state_ref[:, lanes] = state
        slope_ref[:, lanes] = slope_s[row * frames : (row + 1) * frames, :]
        for (top, column), part in zip(spots, parts):
            if column <= row * LANES < column + part.shape[1]:
                x = part[:, row * LANES - column : (row + 1) * LANES - column]
                some = slice(top, top + part.shape[0])
                value = x + valid[some] * state[some]
                if last:
                    rel, at = divmod(row * LANES, outs[0].shape[1])
                    base = top + frames * (rel == 1)
                    out = outs[max(rel - 1, 0)]
                    out[base : base + part.shape[0], at : at + LANES] = value
                else:
                    outs[0][top : top + part.shape[0], lanes] = value


def recur(layer, place, gate, z, stats, params, valid, parts, last):
    frames, features = z.shape
    width = features // 4
    blocks = features // LANES
    whole = lambda array: pl.BlockSpec(array.shape, lambda i: (0,) * array.ndim)
    full = jax.ShapeDtypeStruct((frames, features), F32)
    piece = jax.ShapeDtypeStruct((frames, width), F32)
    outs = [jax.ShapeDtypeStruct((2 * frames, width), F32), piece, piece] if last else [full]
    out_shape = outs + [full, full]
    spread_params = params is None
    if spread_params:
        out_shape.append(jax.ShapeDtypeStruct((3 * LAYERS, blocks, LANES), F32))
        params = valid
    return call(
        partial(recur_body, len(parts), spread_of(parts, width), last, layer, spread_params),
        grid=(1,),
        in_specs=[SMEM_SPEC, SMEM_SPEC]
        + [whole(a) for a in (z, stats, params, valid)]
        + [part_spec(part, frames) for part in parts],
        out_specs=[whole(s) for s in out_shape],
        out_shape=out_shape,
        scratch_shapes=[
            pltpu.VMEM((3, blocks, LANES), F32),
            pltpu.VMEM((blocks, LANES), F32),
        ]
        + [pltpu.VMEM((blocks * frames, LANES), F32)] * 3,
        hbm_outs=(0, 1, 2, 3, 4) if last else (1, 2),
        cost_estimate=cost(100 * frames * features, 20 * frames * features),
        name="recur",
    )(place, gate, in_hbm(z), stats, params, valid, *[in_hbm(a) for a in arrays_of(parts)])


def back_body(n_parts, spots, n_state, layer, place_ref, gate_ref, z_ref, stats_ref, params_ref, *refs):
    parts, refs = refs[:n_parts], refs[n_parts:]
    states, refs = refs[:n_state], refs[n_state:]
    slopes, refs = refs[:n_state], refs[n_state:]
    grad_ref, sums_ref, rows, spread, up_s, state_s, slope_s = refs
    frames = z_ref.shape[0]
    blocks = z_ref.shape[1] // LANES
    tall = frames + 8
    _, mean, inv_std = norm_terms(stats_ref)
    to_relative(place_ref, spread, rows, mean, 0)
    to_relative(place_ref, spread, rows, inv_std, 1)
    for row in range(blocks):
        lanes = slice(row * LANES, (row + 1) * LANES)
        base = row * frames
        up = None
        for (top, column), part in zip(spots, parts):
            if column <= row * LANES < column + part.shape[1] and part.shape[0] == frames:
                value = part[:, row * LANES - column : (row + 1) * LANES - column]
                up = value if up is None else up + value
        up_s[base : base + frames, :] = up
        state_s[row * tall : row * tall + 8, :] = jnp.zeros((8, LANES), F32)
        first = 0
        for state, slope in zip(states, slopes):
            some = state.shape[0]
            at = row * tall + 8 + first
            state_s[at : at + some, :] = state[:, lanes]
            slope_s[base + first : base + first + some, :] = slope[:, lanes]
            first += some
    decay = params_ref[3 * layer + 2]

    def step(i, carry):
        t = frames - 1 - i
        at = pl.ds(t, blocks, stride=frames)
        slope = slope_s[at, :]
        gate = gate_ref[t]
        total = gate * up_s[at, :] + carry
        up_s[at, :] = total * slope
        return total * (slope * decay + (1.0 - gate))

    lax.fori_loop(0, frames, step, jnp.zeros((blocks, LANES), F32), unroll=8)
    per = blocks // 4
    for row in range(blocks):
        lanes = slice(row * LANES, (row + 1) * LANES)
        base = row * frames
        grad = up_s[base : base + frames, :]
        grad_ref[:, lanes] = grad
        zhat = (z_ref[:, lanes] - rows[0, row : row + 1, :]) * rows[1, row : row + 1, :]
        before = state_s[row * tall + 7 : row * tall + 7 + frames, :]
        at = place_ref[row // per] * per + row % per
        for slot, value in enumerate((grad * zhat, grad, grad * before)):
            sums_ref[slot, pl.ds(at, 1), :] = jnp.sum(value, axis=0, keepdims=True)


def spots_of_sum(parts, width):
    spots, column = [], 0
    for array, _ in parts:
        spots.append((0, column % (4 * width)))
        column += array.shape[1]
    return spots


def back(layer, place, gate, z, stats, params, ups, states, slopes):
    frames, features = z.shape
    width = features // 4
    blocks = features // LANES
    whole = lambda array: pl.BlockSpec(array.shape, lambda i: (0,) * array.ndim)
    out_shape = [
        jax.ShapeDtypeStruct((frames, features), F32),
        jax.ShapeDtypeStruct((3, blocks, LANES), F32),
    ]
    z, states, slopes = in_hbm(z), [in_hbm(a) for a in states], [in_hbm(a) for a in slopes]
    return call(
        partial(back_body, len(ups), spots_of_sum(ups, width), len(states), layer),
        grid=(1,),
        in_specs=[SMEM_SPEC] * 2
        + [whole(a) for a in (z, stats, params)]
        + [part_spec(up, frames) for up in ups]
        + [whole(a) for a in (*states, *slopes)],
        out_specs=[whole(a) for a in out_shape],
        out_shape=out_shape,
        scratch_shapes=[
            pltpu.VMEM((2, blocks, LANES), F32),
            pltpu.VMEM((blocks, LANES), F32),
            pltpu.VMEM((blocks * frames, LANES), F32),
            pltpu.VMEM((blocks * (frames + 8), LANES), F32),
            pltpu.VMEM((blocks * frames, LANES), F32),
        ],
        cost_estimate=cost(30 * frames * features, 20 * frames * features),
        name="back",
    )(place, gate, z, stats, params, *arrays_of(ups), *states, *slopes)


def input_terms(high_s, low_s, weights):
    left, right = [], []
    for block, weight in enumerate(weights):
        w_high, w_low = split(weight)
        left += [high_s[block], low_s[block], high_s[block]]
        right += [w_high, w_high, w_low]
    return dot(jnp.concatenate(left, axis=1), jnp.concatenate(right, axis=0), NN)


def norm_back_body(split_terms, layer, cols_ref, place_ref, grad_ref, z_ref, params_ref, valid_ref, stats_ref, sums_ref, *refs):
    del cols_ref
    weights, refs = refs[:10], refs[10:]
    if split_terms:
        out_ref, leave_ref, near_term_ref, far_term_ref, sums_out_ref, *refs = refs
        term_refs, starts = (far_term_ref, near_term_ref), (0, 0)
    else:
        out_ref, leave_ref, term_ref, sums_out_ref, *refs = refs
        term_refs, starts = (term_ref, term_ref), (2 * grad_ref.shape[1] // 4, 0)
    rows, spread, high_s, low_s, far_ref = refs
    blocks = z_ref.shape[1] // LANES
    width = high_s.shape[2]
    per = width // LANES

    @pl.when(pl.program_id(0) == 0)
    def _():
        count, mean, inv_std = norm_terms(stats_ref)
        to_relative(place_ref, spread, rows, mean, 0)
        to_relative(place_ref, spread, rows, inv_std, 1)
        rows[2] = rows[1] * params_ref[3 * layer]
        sums = tree([sums_ref[i : i + 3] for i in range(0, sums_ref.shape[0], 3)])
        sums_out_ref[...] = sums
        to_relative(place_ref, spread, rows, sums[0] / count, 3)
        to_relative(place_ref, spread, rows, sums[1] / count, 4)
        valid = valid_ref[...]
        for row in range(blocks):
            lanes = slice(row * LANES, (row + 1) * LANES)
            one = lambda slot: rows[slot, row : row + 1, :]
            zhat = (z_ref[:, lanes] - one(0)) * one(1)
            value = one(2) * (grad_ref[:, lanes] - valid * (one(4) + zhat * one(3)))
            out_ref[:, lanes] = value
            if (row // per) % 2:
                at = (row // per // 2) * width + (row % per) * LANES
                leave_ref[:, at : at + LANES] = value
            high, low = split(value)
            inner = slice((row % per) * LANES, (row % per + 1) * LANES)
            high_s[row // per, :, inner] = high
            low_s[row // per, :, inner] = low

    value = input_terms(high_s, low_s, weight_blocks(place_ref, weights, far_ref))
    for step, (term_ref, first) in enumerate(zip(term_refs, starts)):

        @pl.when(pl.program_id(0) == step)
        def _():
            for pair in range(2):
                at = pl.multiple_of(((place_ref[0] & 1) ^ pair) * width, width)
                term_ref[:, pl.ds(first + at, width)] = value[
                    :, pair * width : (pair + 1) * width
                ]


def norm_back(columns, place, grad, z, params, valid, stats, sums, weights, layer, split_terms):
    frames, features = z.shape
    width = features // 4
    blocks = features // LANES
    whole = lambda array: pl.BlockSpec(array.shape, lambda s, cols, place: (0,) * array.ndim)
    operands = [grad, in_hbm(z), params, valid, stats, sums]
    full = jax.ShapeDtypeStruct((frames, features), F32)
    half = jax.ShapeDtypeStruct((frames, 2 * width), F32)
    terms = [half, half] if split_terms else [full]
    out_shape = [full, half, *terms, jax.ShapeDtypeStruct((3, blocks, LANES), F32)]
    return call(
        partial(norm_back_body, split_terms, layer),
        grid_spec=pltpu.PrefetchScalarGridSpec(
            num_scalar_prefetch=2,
            grid=(2,),
            in_specs=[whole(a) for a in operands] + weight_specs(weights, layer),
            out_specs=[whole(a) for a in out_shape],
            scratch_shapes=[
                pltpu.VMEM((5, blocks, LANES), F32),
                pltpu.VMEM((blocks, LANES), F32),
                pltpu.VMEM((4, frames, width), BF16),
                pltpu.VMEM((4, frames, width), BF16),
                far_scratch(weights),
            ],
        ),
        out_shape=out_shape,
        hbm_outs=(0,),
        cost_estimate=cost(6 * frames * features * features, 4 * features * features),
        name="norm_back",
    )(columns, place, *operands, *[in_hbm(w) for w in weights])


def own_terms_body(n_ups, spots, cols_ref, place_ref, grad_ref, *refs):
    del cols_ref
    ups, refs = refs[:n_ups], refs[n_ups:]
    weights, refs = refs[:10], refs[10:]
    out_ref, high_s, low_s, far_ref = refs
    width = high_s.shape[2]
    step = pl.program_id(0)

    @pl.when(step == 0)
    def _():
        for block in range(4):
            high, low = split(grad_ref[:, block * width : (block + 1) * width])
            high_s[block] = high
            low_s[block] = low

    value = input_terms(high_s, low_s, weight_blocks(place_ref, weights, far_ref))
    for pair in range(2):
        at = pl.multiple_of(((place_ref[0] & 1) ^ pair) * width, width)
        out_ref[:, pl.ds(at, width)] = value[:, pair * width : (pair + 1) * width]
    for half in range(2):

        @pl.when(step == half)
        def _():
            first = 2 * half * width
            for (_, column), up in zip(spots, ups):
                low = max(column, first)
                high = min(column + up.shape[1], first + 2 * width)
                if low < high:
                    out_ref[:, low - first : high - first] += up[:, low - column : high - column]


def own_terms(columns, place, grad, ups, weights, layer):
    frames, features = grad.shape
    width = features // 4
    whole = lambda array: pl.BlockSpec(array.shape, lambda s, cols, place: (0,) * array.ndim)
    step_block = pl.BlockSpec((frames, 2 * width), lambda s, cols, place: (0, s))
    return call(
        partial(own_terms_body, len(ups), spots_of_sum(ups, width)),
        grid_spec=pltpu.PrefetchScalarGridSpec(
            num_scalar_prefetch=2,
            grid=(2,),
            in_specs=[whole(grad)]
            + [part_spec(up, frames) for up in ups]
            + weight_specs(weights, layer),
            out_specs=step_block,
            scratch_shapes=[pltpu.VMEM((4, frames, width), BF16)] * 2 + [far_scratch(weights)],
        ),
        out_shape=jax.ShapeDtypeStruct((frames, features), F32),
        cost_estimate=cost(6 * frames * features * features, 4 * features * features),
        name="own_terms",
    )(columns, place, in_hbm(grad), *arrays_of(ups), *[in_hbm(w) for w in weights])


def prepare_body(n_chunks, lists_ref, place_ref, *refs):
    del lists_ref
    groups = []
    for _ in range(4):
        groups.append(refs[:n_chunks])
        refs = refs[n_chunks:]
    high_ref, low_ref = refs
    padded = high_ref.shape[0] // 2
    width = high_ref.shape[1] // 2
    for side in range(2):

        @pl.when(pl.program_id(0) // 2 == side)
        def _():
            for clip in range(2):
                for dc in range(2):
                    at = pl.multiple_of((place_ref[6] ^ clip ^ dc) * width, width)
                    row = clip * padded
                    for part in groups[2 * clip + side]:
                        rows = part.shape[0]
                        high, low = split(part[:, dc * width : (dc + 1) * width])
                        high_ref[row : row + rows, pl.ds(at, width)] = high
                        low_ref[row : row + rows, pl.ds(at, width)] = low
                        row += rows
                rest = (clip + 1) * padded - row
                zeros = jnp.zeros((rest, 2 * width), BF16)
                high_ref[row : row + rest, :] = zeros
                low_ref[row : row + rest, :] = zeros


def prepare(lists, place, groups):
    width = groups[0][0].shape[1] // 4
    frames = sum(part.shape[0] for part in groups[0])
    padded = -(-frames // LANES) * LANES
    in_specs = []
    for i, group in enumerate(groups):
        for part in group:
            if i % 2 == 0:
                index = lambda s, *_: (0, jnp.minimum(s, 1))
            else:
                index = lambda s, *_: (0, jnp.maximum(s - 2, 0))
            in_specs.append(pl.BlockSpec((part.shape[0], 2 * width), index))
    out = jax.ShapeDtypeStruct((2 * padded, 8 * width), BF16)
    out_spec = pl.BlockSpec((2 * padded, 2 * width), lambda s, cols, place: (0, cols[s]))
    return call(
        partial(prepare_body, len(groups[0])),
        grid_spec=pltpu.PrefetchScalarGridSpec(
            num_scalar_prefetch=2,
            grid=(4,),
            in_specs=in_specs,
            out_specs=[out_spec, out_spec],
        ),
        out_shape=[out, out],
        hbm_outs=(0, 1),
        cost_estimate=cost(0, 16 * frames * 8 * width),
        name="prepare",
    )(lists, place, *[in_hbm(part) for group in groups for part in group])


def product(g_high, g_low, x_high, x_low):
    return dot(g_high, x_high, NN) + (dot(g_high, x_low, NN) + dot(g_low, x_high, NN))


def weight_body(turn, place_ref, *refs):
    if turn:
        grad_ref, near_ref, x_high, x_low, kept, sent, g_high, g_low, t_high, t_low = refs

        @pl.when(pl.program_id(0) == 0)
        def _():
            frames, features = grad_ref.shape
            width = features // 4
            rows = width // 4
            padded = t_high.shape[1] // 2
            t_high[...] = jnp.zeros_like(t_high)
            t_low[...] = jnp.zeros_like(t_low)
            for clip in range(2):
                for dh in range(2):
                    if clip == 0:
                        part = grad_ref[:, 2 * dh * width : (2 * dh + 1) * width]
                    else:
                        part = near_ref[:, dh * width : (dh + 1) * width]
                    high, low = split(part.T)
                    at = (
                        slice(dh * width, (dh + 1) * width),
                        slice(clip * padded, clip * padded + frames),
                    )
                    t_high[at] = high
                    t_low[at] = low
            for group in range(8):
                first, second, dh = group // 4, group // 2 % 2, group % 2
                core = place_ref[6]
                y = place_ref[4] ^ (first * core + second * (1 - core))
                x = place_ref[5] ^ (first * (1 - core) + second * core)
                at = pl.multiple_of(dh * width + (2 * y + x) * rows, rows)
                g_high[group * rows : (group + 1) * rows, :] = t_high[pl.ds(at, rows), :]
                g_low[group * rows : (group + 1) * rows, :] = t_low[pl.ds(at, rows), :]

    else:
        g_high, g_low, x_high, x_low, kept, sent = refs
    half = g_high.shape[0] // 2
    value = product(g_high[...], g_low[...], x_high[...], x_low[...])
    kept[...] = value[:half].reshape(kept.shape)
    sent[...] = value[half:].reshape(sent.shape)


def weight_rows(half, place, grads, x_split, width):
    turn = half == 0
    whole = lambda array: pl.BlockSpec(array.shape, lambda s, place: (0,) * array.ndim)
    x_spec = pl.BlockSpec((x_split[0].shape[0], width), lambda s, place: (0, 4 * half + s))
    shape = (2, 2, width // 4, 4 * width)
    out_shape = [jax.ShapeDtypeStruct(shape, F32)] * 2
    out_specs = [pl.BlockSpec(shape[:3] + (width,), lambda s, place: (0, 0, 0, s))] * 2
    scratch = []
    if turn:
        turned = (2 * width, x_split[0].shape[0])
        out_shape += [jax.ShapeDtypeStruct(turned, BF16)] * 2
        out_specs += [whole(out_shape[-1])] * 2
        scratch = [pltpu.VMEM(turned, BF16)] * 2
    return call(
        partial(weight_body, turn),
        grid_spec=pltpu.PrefetchScalarGridSpec(
            num_scalar_prefetch=1,
            grid=(4,),
            in_specs=[whole(a) for a in grads] + [x_spec] * 2,
            out_specs=out_specs,
            scratch_shapes=scratch,
        ),
        out_shape=out_shape,
        hbm_outs=(0,),
        cost_estimate=cost(12 * x_split[0].shape[0] * width * 4 * width, 4 * 8 * width * width),
        name="weight_rows",
    )(place, *([in_hbm(grads[0]), grads[1]] if turn else grads), *[in_hbm(x) for x in x_split])


def step_body(n, widths, cut, *refs):
    ins, outs = refs[: 2 * n], refs[2 * n :]
    starts = [sum(widths[:i]) for i in range(len(widths))]
    column = 0
    for i in range(n):
        total = ins[2 * i][...] + ins[2 * i + 1][...]
        end = column + total.shape[-1]
        for j, (start, columns) in enumerate(zip(starts, widths)):
            low, high = max(start, column), min(start + columns, end)
            if low < high:
                to = (Ellipsis, slice(low - start, high - start))
                piece = total[..., low - column : high - column]
                if cut:
                    outs[2 * j][to] = piece[0]
                    outs[2 * j + 1][to] = piece[1]
                else:
                    outs[j][to] = piece
        column = end


def step_of(*pairs, cut=True, widths=None):
    shape = list(pairs[0][0].shape)
    widths = widths or [sum(pair[0].shape[-1] for pair in pairs)]
    outs = []
    for columns in widths:
        shape[-1] = columns
        out = jax.ShapeDtypeStruct(tuple(shape[1:] if cut else shape), F32)
        outs += [out] * (1 + cut)
    whole = lambda array: pl.BlockSpec(array.shape, lambda i: (0,) * array.ndim)
    operands = [array for pair in pairs for array in pair]
    return call(
        partial(step_body, len(pairs), widths, cut),
        grid=(1,),
        in_specs=[whole(a) for a in operands],
        out_specs=[whole(a) for a in outs],
        out_shape=outs,
        cost_estimate=cost(0, 4 * sum(a.size for a in operands)),
        name="reduction_step",
    )(*operands)


def plane_swap(array, step):
    pairs = []
    for i in range(8):
        over_x = (i % 2 == 0) == (step == 0)
        pairs.append((i, i ^ 2 if over_x else i ^ 4))
    return lax.ppermute(array, ("y", "x", "c"), pairs)


def plane_gather(share, *before):
    first = plane_swap(share, 0)
    second = plane_swap(share, 1)
    return [share, second, first, plane_swap(after(first, *before), 1)]


def assemble_body(groups, place_ref, *refs):
    out_ref = refs[-1]
    core = place_ref[6]
    column = 0
    for group in range(groups):
        rows, columns = refs[4 * group].shape
        for i in range(4):
            first, second = i // 2, i % 2
            y = place_ref[4] ^ (first * core + second * (1 - core))
            x = place_ref[5] ^ (first * (1 - core) + second * core)
            at = pl.multiple_of((2 * y + x) * rows, rows)
            out_ref[0, pl.ds(at, rows), column : column + columns] = refs[4 * group + i][...]
        column += columns


def assemble(place, groups, layer, onto=None):
    pieces = [piece for group in groups for piece in group]
    rows = 4 * pieces[0].shape[0]
    columns = sum(group[0].shape[1] for group in groups)
    aliases, extra, extra_specs = {}, [], []
    if onto is not None:
        aliases, extra = {1 + len(pieces): 0}, [onto]
        extra_specs = [pl.BlockSpec(memory_space=pl.ANY)]
    (out,) = call(
        partial(assemble_body, len(groups)),
        grid=(1,),
        out_shape=[jax.ShapeDtypeStruct((LAYERS, rows, columns), F32)],
        hbm_outs=(0,),
        in_specs=[SMEM_SPEC]
        + [pl.BlockSpec(p.shape, lambda i: (0, 0)) for p in pieces]
        + extra_specs,
        out_specs=[pl.BlockSpec((1, rows, columns), lambda i: (layer, 0, 0))],
        input_output_aliases=aliases,
        cost_estimate=cost(0, 8 * rows * columns),
        name="assemble",
    )(place, *[p if extra else in_hbm(p) for p in pieces], *extra)
    return out


def half_features(inputs, weights, gains, shifts, decays, biases, lengths, frame_mask, grad_out):
    width, slots = inputs.shape
    clips, frames = frame_mask.shape
    depth = weights.shape[2]
    blocks = 4 * width // LANES
    y, x, h, l, c = (lax.axis_index(name) for name in ("y", "x", "h", "l", "c"))
    b = 2 * y + x
    numbers = [2 * (h ^ (rel // 2)) + (c ^ (rel % 2)) for rel in range(4)] + [y, x, c]
    place = jnp.stack(numbers).astype(jnp.int32)
    own_blocks, other_blocks = (
        jnp.stack(
            [2 * (2 * (h ^ (rel // 2)) + half) + (c ^ (rel % 2)) for rel in range(4)]
        ).astype(jnp.int32)
        for half in (l, 1 - l)
    )
    own_columns = jnp.stack([2 * h + l, 2 * (1 - h) + l]).astype(jnp.int32)
    other_columns = jnp.stack([2 * (1 - h) + 1 - l, 2 * h + 1 - l]).astype(jnp.int32)
    all_columns = jnp.concatenate([own_columns, other_columns[::-1]])
    rows = width // 4

    clip = 2 * h + c
    seen = lax.dynamic_index_in_dim(frame_mask, clip, 0, keepdims=False)
    length = lax.dynamic_index_in_dim(lengths, clip, 0, keepdims=False)
    moments = jnp.arange(frames, dtype=jnp.int32)
    gate = ((moments < length) & ((seen == 1) | (moments == 0))).astype(F32)
    valid = jnp.broadcast_to(gate[:, None], (frames, LANES))

    def far_share(layer):
        return lax.dynamic_slice(weights, (layer, b * rows, 0), (1, rows, depth))[0]

    def over_h(array):
        return lax.ppermute(array, "h", FLIP2)

    def over_c(array):
        return lax.ppermute(array, "c", FLIP2)

    def over_second(array):
        return plane_swap(array, 1)

    def four_of(near_rows, far_rows):
        return [
            (near_rows, 0),
            (over_c(near_rows), 1),
            (far_rows, 0),
            (over_c(far_rows), 1),
        ]

    def far_pieces(share):
        both = lax.ppermute(share, ("y", "x"), DIAGONAL)
        return [share, lax.ppermute(share, "x", FLIP2), lax.ppermute(share, "y", FLIP2), both]

    near = over_c(weights)
    share = far_share(0)
    close, away = pack(place, after(inputs, share), frames)
    share = over_h(share)
    away = over_h(away)
    other_close = swap_half(close)
    up_close, up_away = pack(place, after(grad_out, close), frames, waits=True)
    share = after(share, up_close, valid, near, other_close)
    pieces = far_pieces(share)
    away = after(away, pieces[1:])
    half_weights = [[weights, near, *pieces, *map(over_c, after(pieces, away))]]
    own = four_of(after(close, away), away)
    other_away = swap_half(away)
    params = jnp.stack([gains, shifts + biases, decays], axis=1)
    own_params = params.reshape(LAYERS * 3 * width // LANES, LANES)
    params = None

    saved = []
    for layer in range(LAYERS):
        last = layer == LAYERS - 1
        flat = layer == 0
        if layer > 0:
            others = [(swap_half(array), None) for array, _ in own]
        z, *own_flat = project(
            own_blocks, place, frames, own, half_weights[layer], layer, flat=flat
        )
        if flat:
            others = four_of(other_close, after(other_away, z))
        z, stats, *other_flat = project(
            other_blocks,
            place,
            frames,
            others,
            half_weights[layer],
            layer,
            z,
            valid,
            own_params if flat else None,
            flat,
        )
        if last:
            upstream = four_of(up_close, after(up_away, z))
        if flat:
            stats = lax.all_gather(stats, ("h", "c"), tiled=True)
            share = over_h(after(far_share(1), stats))
            stats = lax.all_gather(stats, ("y", "x"), tiled=True)
        else:
            stats = lax.all_gather(stats, ("y", "x"), tiled=True)
            stats = lax.all_gather(stats, ("h", "c"), tiled=True)
        if flat:
            own = [(own_flat[0], None)]
        *following, states, slopes = recur(
            layer, place, gate, z, stats, params, valid, own, last
        )
        if flat:
            *following, states, slopes, params = *following, states, slopes
            groups = [own_flat, other_flat]
        else:
            groups = [arrays_of(own), arrays_of(others)]
        groups += [[over_c(after(p, z)) for p in group] for group in groups]
        x_split = prepare(all_columns, place, after(groups, slopes)) if flat else None
        if flat:
            up_away = over_h(after(up_away, x_split[0]))
            pieces = far_pieces(after(share, slopes))
            half_weights.append([weights, near, *pieces, *map(over_c, pieces)])
        saved.append((groups, x_split, z, stats, states, slopes))
        own = [(array, None) for array in following]
    output, away, diagonal = following
    diagonal = over_c(over_h(diagonal))

    ups = upstream
    results = [None] * LAYERS
    for layer in range(LAYERS - 1, -1, -1):
        groups, x_split, z, stats, states, slopes = saved[layer]
        weight = half_weights[layer]
        grad_pre, sums = back(
            layer, place, gate, z, stats, params, ups, [states], [slopes]
        )
        plane = lax.all_gather(sums, ("y", "x"), tiled=True)
        if layer == 0:
            later, go = step_of(*[(in_hbm(k), after(g, plane)) for k, g in zip(stay, come)])
            plane = after(plane, later)
            go = over_second(go)
        sums = lax.all_gather(plane, ("h", "c"), tiled=True)
        if layer > 0:
            away = over_h(after(away, sums))
        grad_z, leaving, *terms, sums = norm_back(
            other_columns, place, grad_pre, z, params, valid, stats, sums, weight, layer,
            layer == 0,
        )
        leaving = over_c(leaving)
        if layer > 0:
            received = [swap_half(terms[0])]
            x_split = prepare(all_columns, place, after(groups, grad_z, diagonal))
        else:
            received = [None, swap_half(terms[1])]
            later, go = step_of((later, after(go, grad_z)))
            leaving = after(leaving, later)
            later = (later, over_h(go))
        *first, g_high, g_low = weight_rows(0, place, (grad_z, leaving), x_split, width)
        turned = (g_high, g_low)
        come = [plane_swap(first[1], 0)]
        if layer > 0:
            turned = after(turned, away)
            output = [(output, 0), (over_c(output), 1), (away, 0), (diagonal, 0)]
        else:
            received[0] = swap_half(after(terms[0], received[1]))
        second = weight_rows(1, place, turned, x_split, width)
        come.append(plane_swap(second[1], 0))
        stay = (first[0], second[0])
        kept = own_terms(own_columns, place, after(grad_z, second[0]), ups, weight, layer)
        ups = [(kept, None)] + [(r, None) for r in received]
        results[layer] = lax.dynamic_index_in_dim(
            sums.reshape(3, 4, width), clip, axis=1, keepdims=False
        )

    away = merge(kept, 1, received[1])
    (later,) = step_of((later[0], after(later[1], away)), cut=False)
    away = over_h(away)
    later_first, later_second = plane_swap(later, 0), plane_swap(later, 1)
    total, go = step_of((in_hbm(stay[0]), after(come[0], later_first)), (in_hbm(stay[1]), come[1]))
    go = over_second(go)
    later = [later, later_second, later_first, plane_swap(after(later_first, total), 1)]
    far = [(away, 0), (over_c(away), 1)]
    total, go = step_of((total, after(go, far[1][0])))
    go = over_h(go)
    output = unpack(place, [(after(array, total), i) for array, i in output], frames, waited=True)
    grad_weights = assemble(place, after([later], output), 1)
    (share,) = step_of((total, after(go, grad_weights)), cut=False)
    gathered = plane_gather(share)
    close = merge(kept, 0, after(received[0], gathered[2]))
    grad_in = [(close, 0), (over_c(close[frames:]), 0)] + far
    grad_in = unpack(place, grad_in, frames)
    grad_weights = assemble(place, after([gathered], grad_in), 0, grad_weights)
    sums = jnp.stack(results)
    return (
        output,
        grad_in,
        grad_weights,
        sums[:, 0],
        sums[:, 1],
        sums[:, 2],
        sums[:, 1],
    )


def gelu_slope(value):
    return (
        0.5 * (1.0 + jax.scipy.special.erf(value / ROOT_TWO))
        + value * jnp.exp(-0.5 * value * value) / ROOT_TWO_PI
    )


def recur_step(decay, state, inputs):
    drive_t, valid_t = inputs
    pre = drive_t + decay * state
    state = state + valid_t * (jax.nn.gelu(pre, approximate=False) - state)
    return (state, state)


def back_step(decay, carry, inputs):
    upstream_t, valid_t, pre_t = inputs
    total = upstream_t + carry
    grad_pre = total * valid_t * gelu_slope(pre_t)
    carry = total * (1.0 - valid_t) + grad_pre * decay
    return (carry, grad_pre)


def add_piece(weight, piece):
    return jnp.dot(weight, piece, precision=HIGH, preferred_element_type=jnp.float32)


def weight_columns(grad_pre_norm, piece):
    return jnp.einsum("jf,kf->jk", grad_pre_norm, piece, precision=HIGH)


def split_features(inputs, weights, gains, shifts, decays, biases, lengths, frame_mask, grad_out):
    width, slots = inputs.shape
    clips, frames_len = frame_mask.shape
    frames = jnp.arange(frames_len, dtype=jnp.int32)
    valid_grid = (
        (frames[None, :] < lengths[:, None]) & ((frame_mask == 1) | (frames[None, :] == 0))
    ).astype(jnp.float32)
    valid = valid_grid.reshape(-1)
    valid_row = valid[None, :]
    valid_time = jnp.broadcast_to(valid_grid.T[:, :, None], (frames_len, clips, width)).reshape(
        frames_len, clips * width
    )
    count_local = jnp.sum(valid)

    def to_time(array):
        return jnp.transpose(array.reshape(width, clips, frames_len), (2, 1, 0)).reshape(
            frames_len, clips * width
        )

    def from_time(array):
        return jnp.transpose(array.reshape(frames_len, clips, width), (2, 1, 0)).reshape(
            width, slots
        )

    layer_in = inputs
    saved = []
    for layer_no in range(LAYERS):
        weight = weights[layer_no]
        gathered = lax.all_gather(layer_in, "neuron", axis=0, tiled=True)
        pre_norm = add_piece(weight, gathered)
        first_sum, count = lax.psum((jnp.sum(valid_row * pre_norm, axis=1), count_local), "batch")
        mean = first_sum / count
        centered = pre_norm - mean[:, None]
        var = lax.psum(jnp.sum(valid_row * centered * centered, axis=1), "batch") / count
        inv_std = lax.rsqrt(var + EPS)
        zhat = (pre_norm - mean[:, None]) * inv_std[:, None]
        drive = gains[layer_no][:, None] * zhat + (shifts[layer_no] + biases[layer_no])[:, None]
        drive_time = to_time(drive)
        decay_wide = jnp.tile(decays[layer_no], clips)
        start_state = jnp.zeros((clips * width,), jnp.float32)
        _, states = lax.scan(
            partial(recur_step, decay_wide), start_state, (drive_time, valid_time), unroll=8
        )
        saved.append((gathered, zhat, inv_std, drive_time, states, count))
        layer_in = layer_in + valid_row * from_time(states)
    upstream = grad_out
    grad_parts = [None] * LAYERS
    for layer_no in range(LAYERS - 1, -1, -1):
        gathered, zhat, inv_std, drive_time, states, count = saved[layer_no]
        decay_wide = jnp.tile(decays[layer_no], clips)
        gain = gains[layer_no]
        previous = jnp.concatenate([jnp.zeros_like(states[:1]), states[:-1]], axis=0)
        pre_time = drive_time + decay_wide[None, :] * previous
        grad_state = to_time(valid_row * upstream)
        start_carry = jnp.zeros((clips * width,), jnp.float32)
        _, grad_pre_time = lax.scan(
            partial(back_step, decay_wide),
            start_carry,
            (grad_state, valid_time, pre_time),
            reverse=True,
            unroll=8,
        )
        decay_local = jnp.sum(
            jnp.sum(grad_pre_time * previous, axis=0).reshape(clips, width), axis=0
        )
        grad_pre = from_time(grad_pre_time)
        gain_local = jnp.sum(grad_pre * zhat, axis=1)
        shift_local = jnp.sum(grad_pre, axis=1)
        grad_gain, grad_shift, grad_decay = lax.psum(
            (gain_local, shift_local, decay_local), "batch"
        )
        grad_pre_norm = (gain * inv_std)[:, None] * (
            grad_pre - valid_row * (grad_shift[:, None] + zhat * grad_gain[:, None]) / count
        )
        weight_local = weight_columns(grad_pre_norm, gathered)
        input_terms = jnp.einsum("jk,jf->kf", weights[layer_no], grad_pre_norm, precision=HIGH)
        input_grad = lax.psum_scatter(input_terms, "neuron", scatter_dimension=0, tiled=True)
        grad_weight = lax.psum(weight_local, "batch")
        upstream = upstream + input_grad
        grad_parts[layer_no] = (grad_weight, grad_gain, grad_shift, grad_decay)
    grad_weights = jnp.stack([grad_parts[layer_no][0] for layer_no in range(LAYERS)])
    grad_gains = jnp.stack([grad_parts[layer_no][1] for layer_no in range(LAYERS)])
    grad_shifts = jnp.stack([grad_parts[layer_no][2] for layer_no in range(LAYERS)])
    grad_decays = jnp.stack([grad_parts[layer_no][3] for layer_no in range(LAYERS)])
    return (layer_in, upstream, grad_weights, grad_gains, grad_shifts, grad_decays, grad_shifts)


def solution(mesh):
    if (mesh.shape["batch"], mesh.shape["neuron"]) == (4, 8):
        cut = Mesh(mesh.devices.reshape(2, 2, 2, 2, 2), ("y", "x", "h", "l", "c"))
        batch, neuron, body = ("y", "x"), ("h", "l", "c"), half_features
    else:
        cut, batch, neuron, body = mesh, "batch", "neuron", split_features
    in_specs = (
        P(neuron, batch),
        P(None, neuron, None),
        P(None, neuron),
        P(None, neuron),
        P(None, neuron),
        P(None, neuron),
        P(batch),
        P(batch, None),
        P(neuron, batch),
    )
    out_specs = (
        P(neuron, batch),
        P(neuron, batch),
        P(None, neuron, None),
        P(None, neuron),
        P(None, neuron),
        P(None, neuron),
        P(None, neuron),
    )
    return jax.shard_map(
        body, mesh=cut, in_specs=in_specs, out_specs=out_specs, check_vma=False
    )
```

```python
from functools import partial
import math

import jax
import jax.numpy as jnp
from jax import lax
from jax.experimental import pallas as pl
from jax.experimental.pallas import tpu as pltpu
from jax.sharding import Mesh, PartitionSpec as P

LAYERS = 2
EPS = 1e-05
HIGH = lax.Precision.HIGHEST
ROOT_TWO = math.sqrt(2.0)
ROOT_TWO_PI = math.sqrt(2.0 * math.pi)
F32 = jnp.float32
BF16 = jnp.bfloat16
LANES = 128
VMEM_LIMIT = 24 * 1024 * 1024
SMEM_SPEC = pl.BlockSpec(memory_space=pltpu.SMEM)
VMEM_SPEC = pl.BlockSpec(memory_space=pltpu.VMEM)


FLIP2 = [(0, 1), (1, 0)]
DIAGONAL = [(0, 3), (1, 2), (2, 1), (3, 0)]


def swap_half(array):
    return lax.ppermute(array, "l", FLIP2)


def after(value, *others):
    return lax.optimization_barrier((value, others))[0]


def split(value):
    high = value.astype(BF16)
    return high, (value - high.astype(F32)).astype(BF16)


def dot(a, b, dims):
    return lax.dot_general(a, b, (dims, ((), ())), preferred_element_type=F32)


NT = ((1,), (1,))
NN = ((1,), (0,))


def in_hbm(array):
    return pltpu.with_memory_space_constraint(array, pltpu.HBM)


def call(body, out_shape, hbm_outs=(), **kwargs):
    if hbm_outs:
        out_shape = [
            pltpu.HBM(a.shape, a.dtype) if i in hbm_outs else a for i, a in enumerate(out_shape)
        ]
    return pl.pallas_call(
        body,
        out_shape=out_shape,
        compiler_params=pltpu.CompilerParams(vmem_limit_bytes=VMEM_LIMIT),
        **kwargs,
    )


def cost(flops, byte_count):
    return pl.CostEstimate(flops=int(flops) // 64, bytes_accessed=int(byte_count) // 64, transcendentals=0)


def pack_body(frames, place_ref, in_ref, near_ref, far_ref, turned):
    slots = in_ref.shape[1]
    for start in range(0, slots, LANES):
        turned[start : start + LANES, :] = in_ref[:, start : start + LANES].T
    for rel in range(4):
        first = pl.multiple_of(place_ref[rel] * frames, 8)
        out = (near_ref, far_ref)[rel // 2]
        out[(rel % 2) * frames : (rel % 2 + 1) * frames, :] = turned[pl.ds(first, frames), :]


def pack(place, array, frames, waits=False):
    width, slots = array.shape
    out = jax.ShapeDtypeStruct((2 * frames, width), F32)
    return call(
        partial(pack_body, frames),
        grid=(1,),
        out_shape=[out, out],
        in_specs=[SMEM_SPEC, pl.BlockSpec((width, slots), lambda i: (0, 0))],
        out_specs=[pl.BlockSpec(out.shape, lambda i: (0, 0))] * 2,
        scratch_shapes=[pltpu.VMEM((slots, width), F32)],
        hbm_outs=(0, 1) if waits else (),
        cost_estimate=cost(0, 8 * width * slots),
        name="pack",
    )(place, in_hbm(array))


def part_spec(part, frames):
    array, i = part
    if i is None:
        return pl.BlockSpec(array.shape, lambda *_: (0,) * array.ndim)
    return pl.BlockSpec((frames, array.shape[1]), lambda *_: (i, 0))


def arrays_of(parts):
    return [array for array, _ in parts]


def unpack_body(frames, place_ref, *refs):
    ins, out_ref, turned = refs[:4], refs[4], refs[5]
    slots = out_ref.shape[1]
    for rel in range(4):
        first = pl.multiple_of(place_ref[rel] * frames, 8)
        turned[pl.ds(first, frames), :] = ins[rel][...]
    for start in range(0, slots, LANES):
        out_ref[:, start : start + LANES] = turned[start : start + LANES, :].T


def unpack(place, parts, frames, waited=False):
    width = parts[0][0].shape[1]
    slots = 4 * frames
    return call(
        partial(unpack_body, frames),
        grid=(1,),
        out_shape=jax.ShapeDtypeStruct((width, slots), F32),
        in_specs=[SMEM_SPEC] + [part_spec(part, frames) for part in parts],
        out_specs=pl.BlockSpec((width, slots), lambda i: (0, 0)),
        scratch_shapes=[pltpu.VMEM((slots, width), F32)],
        cost_estimate=cost(0, 8 * width * slots),
        name="unpack",
    )(place, *[in_hbm(a) if waited else a for a in arrays_of(parts)])


def merge_body(kept_ref, come_ref, out_ref):
    frames, columns = kept_ref.shape
    width = columns // 2
    for i in range(2):
        some = slice(i * width, (i + 1) * width)
        out_ref[i * frames : (i + 1) * frames, :] = kept_ref[:, some] + come_ref[:, some]


def merge(kept, half, come):
    frames, columns = come.shape
    return call(
        merge_body,
        grid=(1,),
        out_shape=jax.ShapeDtypeStruct((2 * frames, columns // 2), F32),
        in_specs=[
            pl.BlockSpec((frames, columns), lambda i: (0, half)),
            pl.BlockSpec((frames, columns), lambda i: (0, 0)),
        ],
        out_specs=pl.BlockSpec((2 * frames, columns // 2), lambda i: (0, 0)),
        cost_estimate=cost(0, 12 * frames * columns),
        name="merge",
    )(kept, come)


def project_body(n_parts, n_flat, spots, n_weights, first, with_acc, with_stats, with_params, cols_ref, place_ref, *refs):
    del cols_ref

    def take(n):
        nonlocal refs
        some, refs = refs[:n], refs[n:]
        return some

    parts, flat_parts, weights = take(n_parts), take(n_flat), take(n_weights)
    acc, valid, stats_in, params = take(with_acc), take(with_stats > 0), take(with_stats > 1), take(with_params)
    (out_ref,) = take(1)
    stats, flat = take(with_stats > 0), take(n_flat > 0)
    x_high, x_low, far_ref = refs
    step = pl.program_id(0)
    width = x_high.shape[2]

    @pl.when(step == 0)
    def _():
        for block, part in zip(spots, parts):
            for start in range(0, part.shape[1], width):
                high, low = split(part[:, start : start + width])
                x_high[block + start // width] = high
                x_low[block + start // width] = low
        column = 0
        for part in flat_parts:
            flat[0][:, column : column + part.shape[1]] = part[...]
            column += part.shape[1]
        if with_acc:
            out_ref[...] = acc[0][...]
        else:
            out_ref[...] = jnp.zeros_like(out_ref)

    stacked = jnp.concatenate([x_high[step], x_low[step], x_high[step]], axis=1)
    for block, weight in enumerate(weight_blocks(place_ref, weights, far_ref)):
        w_high, w_low = split(weight)
        columns = slice(block * width, (block + 1) * width)
        out_ref[:, columns] += dot(stacked, jnp.concatenate([w_high, w_high, w_low], axis=1), NT)

    if with_stats:
        (stats_ref,) = stats

        @pl.when(step == pl.num_programs(0) - 1)
        def _():
            if stats_in:
                stats_ref[...] = stats_in[0][...]
            own = jnp.sum(valid[0][...], axis=0, keepdims=True)
            per = width // LANES
            for row in range(out_ref.shape[1] // LANES):
                z = out_ref[:, row * LANES : (row + 1) * LANES]
                total = jnp.sum(valid[0][...] * z, axis=0, keepdims=True)
                centred = valid[0][...] * (z - total / own)
                squares = jnp.sum(centred * centred, axis=0, keepdims=True)
                at = place_ref[first + row // per] * per + row % per
                stats_ref[0, pl.ds(at, 1), :] = total
                stats_ref[1, pl.ds(at, 1), :] = squares
                stats_ref[2, pl.ds(at, 1), :] = own
            if with_params:
                rest = params[0].shape[0] - 8
                stats_ref[3] = params[0][:8, :]
                stats_ref[4] = jnp.zeros_like(stats_ref[4])
                stats_ref[4, :rest, :] = params[0][8:, :]


def weight_specs(weights, layer, pairs=2):
    specs = []
    for weight in weights:
        if weight.ndim == 3:
            shape = (1, weight.shape[1], pairs * weight.shape[1])
            specs.append(pl.BlockSpec(shape, lambda s, cols, *_: (layer, 0, cols[s])))
        else:
            shape = (weight.shape[0], pairs * 4 * weight.shape[0])
            specs.append(pl.BlockSpec(shape, lambda s, cols, *_: (0, cols[s])))
    return specs


def far_scratch(width, pairs=2):
    return pltpu.VMEM((2, width, pairs * width), F32)


def weight_blocks(place_ref, refs, far_ref):
    near = [ref[0] for ref in refs if len(ref.shape) == 3]
    pieces = [ref for ref in refs if len(ref.shape) == 2]
    far = []
    for i in range(len(pieces) // 4):
        for rel, piece in enumerate(pieces[4 * i : 4 * i + 4]):
            rows = piece.shape[0]
            row = 2 * (place_ref[4] ^ (rel // 2)) + (place_ref[5] ^ (rel % 2))
            far_ref[i, pl.ds(pl.multiple_of(row * rows, rows), rows), :] = piece[...]
        far.append(far_ref[i])
    return near + far


def project(
    place, frames, parts, blocks, weights, layer, acc=None, valid=None, stats=None, params=None, flat=()
):
    near = weights[0].ndim == 3
    units = sum(1 if w.ndim == 3 else 0.25 for w in weights)
    width = weights[0].shape[1] if near else 4 * weights[0].shape[0]
    n = blocks.shape[0]
    spots, block = [], 0
    for array, _ in parts:
        spots.append(block)
        block += array.shape[1] // width
    full = pl.BlockSpec(memory_space=pltpu.VMEM)
    in_specs = [part_spec(part, frames) for part in (*parts, *flat)]
    in_specs += weight_specs(weights, layer, 1)
    operands = arrays_of(parts) + arrays_of(flat) + [in_hbm(w) for w in weights]
    array = jax.ShapeDtypeStruct((frames, int(units) * width), F32)
    array_spec = pl.BlockSpec(array.shape, lambda s, cols, place: (0, 0))
    out_shape, out_specs = [array], [array_spec]
    if acc is not None:
        in_specs.append(array_spec)
        operands.append(in_hbm(acc))
    if valid is not None:
        in_specs.append(full)
        operands.append(valid)
        shape = (3 if params is None else 5, 4 * width // LANES, LANES)
        out_shape.append(jax.ShapeDtypeStruct(shape, F32))
        out_specs.append(pl.BlockSpec(shape, lambda s, cols, place: (0, 0, 0)))
    for extra in (stats, params):
        if extra is not None:
            in_specs.append(full)
            operands.append(extra)
    if flat:
        out_shape.append(jax.ShapeDtypeStruct((frames, 4 * width), F32))
        out_specs.append(pl.BlockSpec((frames, 4 * width), lambda s, cols, place: (0, 0)))
    return call(
        partial(
            project_body,
            len(parts),
            len(flat),
            spots,
            len(weights),
            0 if near else 2,
            acc is not None,
            (valid is not None) + (stats is not None),
            params is not None,
        ),
        grid_spec=pltpu.PrefetchScalarGridSpec(
            num_scalar_prefetch=2,
            grid=(n,),
            in_specs=in_specs,
            out_specs=out_specs,
            scratch_shapes=[pltpu.VMEM((n, frames, width), BF16)] * 2 + [far_scratch(width, 1)],
        ),
        out_shape=out_shape,
        hbm_outs=(0, len(out_shape) - 1) if flat else (0,),
        cost_estimate=cost(6 * frames * n * width * units * width, 4 * n * width * units * width),
        name="project",
    )(blocks, place, *operands)


def to_relative(place_ref, spread, rows_ref, value, slot):
    per = value.shape[0] // 4
    spread[...] = value
    for rel in range(4):
        first = place_ref[rel] * per
        for row in range(per):
            rows_ref[slot, rel * per + row : rel * per + row + 1, :] = spread[
                pl.ds(first + row, 1), :
            ]


def tree(values):
    while len(values) > 1:
        values = [a + b for a, b in zip(values[::2], values[1::2])]
    return values[0]


def gathered(refs, slot):
    step = refs[0].shape[0] // 8
    return [ref[i] for i in range(slot, refs[0].shape[0], step) for ref in refs]


def norm_terms(stats_refs):
    each = [gathered(stats_refs, slot) for slot in range(3)]
    totals, squares, owns = each
    count = tree(owns)
    mean = tree(totals) / count
    away = [total / own - mean for total, own in zip(totals, owns)]
    spread = tree([s + n * a * a for s, n, a in zip(squares, owns, away)])
    return count, mean, lax.rsqrt(spread / count + EPS)


CHUNKS = 4


def columns_of(refs, row):
    for ref in refs:
        if row * LANES < ref.shape[1]:
            return ref[:, row * LANES : (row + 1) * LANES]
        row -= ref.shape[1] // LANES


def recur_body(n_z, last, layer, spread_params, place_ref, gate_ref, *refs):
    z_refs, refs = refs[:n_z], refs[n_z:]
    stats_refs, (params_ref, valid_ref, x_ref), refs = refs[:2], refs[2:5], refs[5:]
    outs, refs = refs[: 1 + 3 * last], refs[1 + 3 * last :]
    if spread_params:
        state_ref, slope_ref, params_out, rows, spread, held, drive_s, state_s, slope_s = refs
    else:
        state_ref, slope_ref, rows, spread, held, drive_s, state_s, slope_s = refs
    frames, features = x_ref.shape
    blocks = features // LANES
    per = blocks // 4
    chunk = pl.program_id(0)

    @pl.when(chunk == 0)
    def _():
        if spread_params:
            step = stats_refs[0].shape[0] // 8
            for rel in range(4):
                first = (place_ref[rel] >> 1) * step + 3
                for row in range(LAYERS * 3 * per):
                    at = rel * per + row % per
                    params_out[row // per, at : at + 1, :] = stats_refs[rel % 2][
                        first + row // 8, row % 8 : row % 8 + 1, :
                    ]
            params = [params_out[3 * layer + i] for i in range(3)]
        else:
            params = [params_ref[3 * layer + i] for i in range(3)]
        _, mean, inv_std = norm_terms(stats_refs)
        to_relative(place_ref, spread, rows, mean, 0)
        to_relative(place_ref, spread, rows, inv_std, 1)
        rows[1] = rows[1] * params[0]
        rows[2] = params[1]
        rows[3] = params[2]
        held[...] = jnp.zeros_like(held)

    for row in range(blocks):
        drive_s[row * frames : (row + 1) * frames, :] = (
            columns_of(z_refs, row) - rows[0, row : row + 1, :]
        ) * rows[1, row : row + 1, :] + rows[2, row : row + 1, :]
    decay = rows[3]

    def step(t, state):
        at = pl.ds(t, blocks, stride=frames)
        pre = drive_s[at, :] + decay * state
        half = 0.5 + 0.5 * lax.erf(pre * (1.0 / ROOT_TWO))
        gate = gate_ref[chunk * frames + t] > 0.0
        slope = half + pre * jnp.exp(-0.5 * pre * pre) * (1.0 / ROOT_TWO_PI)
        state = jnp.where(gate, pre * half, state)
        state_s[at, :] = state
        slope_s[at, :] = jnp.where(gate, slope, 0.0)
        return state

    held[...] = lax.fori_loop(0, frames, step, held[...], unroll=8)
    valid = valid_ref[...]
    for row in range(blocks):
        lanes = slice(row * LANES, (row + 1) * LANES)
        state = state_s[row * frames : (row + 1) * frames, :]
        state_ref[:, lanes] = state
        slope_ref[:, lanes] = slope_s[row * frames : (row + 1) * frames, :]
        value = x_ref[:, lanes] + valid * state
        out, at = (outs[row // per], row % per) if last else (outs[0], row)
        out[:, at * LANES : (at + 1) * LANES] = value


def recur(layer, place, gate, z, stats, params, valid, x, last):
    frames, features = x.shape
    blocks = features // LANES
    some = frames // CHUNKS
    whole = lambda array: pl.BlockSpec(array.shape, lambda i: (0,) * array.ndim)
    by_chunk = lambda array: pl.BlockSpec((some, array.shape[1]), lambda i: (i, 0))
    full = jax.ShapeDtypeStruct((frames, features), F32)
    piece = jax.ShapeDtypeStruct((frames, features // 4), F32)
    out_shape = [piece] * 4 if last else [full]
    out_shape += [full, full]
    out_specs = [by_chunk(a) for a in out_shape]
    spread_params = params is None
    if spread_params:
        out_shape.append(jax.ShapeDtypeStruct((3 * LAYERS, blocks, LANES), F32))
        out_specs.append(whole(out_shape[-1]))
        params = valid
    return call(
        partial(recur_body, len(z), last, layer, spread_params),
        grid=(CHUNKS,),
        in_specs=[SMEM_SPEC, SMEM_SPEC]
        + [by_chunk(a) for a in z]
        + [whole(a) for a in (*stats, params)]
        + [by_chunk(a) for a in (valid, x)],
        out_specs=out_specs,
        out_shape=out_shape,
        hbm_outs=tuple(range(len(out_shape) - spread_params)) if last else (1, 2),
        scratch_shapes=[
            pltpu.VMEM((4, blocks, LANES), F32),
            pltpu.VMEM((blocks, LANES), F32),
            pltpu.VMEM((blocks, LANES), F32),
        ]
        + [pltpu.VMEM((blocks * some, LANES), F32)] * 3,
        cost_estimate=cost(100 * frames * features, 20 * frames * features),
        name="recur",
    )(place, gate, *[in_hbm(a) for a in z], *stats, params, valid, in_hbm(x))


def back_body(n_z, n_ups, spots, layer, place_ref, gate_ref, *refs):
    z_refs, refs = refs[:n_z], refs[n_z:]
    stats_refs, params_ref, refs = refs[:2], refs[2], refs[3:]
    ups, (state_ref, slope_ref), refs = refs[:n_ups], refs[n_ups : n_ups + 2], refs[n_ups + 2 :]
    grad_ref, sums_ref, rows, spread, held, up_s, state_s, slope_s = refs
    frames, features = state_ref.shape
    blocks = features // LANES
    per = blocks // 4
    tall = frames + 8
    step_no = pl.program_id(0)
    chunk = pl.num_programs(0) - 1 - step_no

    @pl.when(step_no == 0)
    def _():
        _, mean, inv_std = norm_terms(stats_refs)
        to_relative(place_ref, spread, rows, mean, 0)
        to_relative(place_ref, spread, rows, inv_std, 1)
        held[...] = jnp.zeros_like(held)

    for row in range(blocks):
        lanes = slice(row * LANES, (row + 1) * LANES)
        base = row * frames
        up = None
        for (_, column), part in zip(spots, ups):
            if column <= row * LANES < column + part.shape[1]:
                value = part[:, row * LANES - column : (row + 1) * LANES - column]
                up = value if up is None else up + value
        up_s[base : base + frames, :] = up
        state_s[row * tall : row * tall + 8, :] = jnp.zeros((8, LANES), F32)
        state_s[row * tall + 8 : (row + 1) * tall, :] = state_ref[:, lanes]
        slope_s[base : base + frames, :] = slope_ref[:, lanes]
    decay = params_ref[3 * layer + 2]

    def step(i, carry):
        t = frames - 1 - i
        at = pl.ds(t, blocks, stride=frames)
        slope = slope_s[at, :]
        gate = gate_ref[chunk * frames + t]
        total = gate * up_s[at, :] + carry
        up_s[at, :] = total * slope
        return total * (slope * decay + (1.0 - gate))

    held[0] = lax.fori_loop(0, frames, step, held[0], unroll=8)
    held[4] += held[1] * state_s[pl.ds(tall - 1, blocks, stride=tall), :]
    held[1] = up_s[pl.ds(0, blocks, stride=frames), :]
    for row in range(blocks):
        lanes = slice(row * LANES, (row + 1) * LANES)
        grad = up_s[row * frames : (row + 1) * frames, :]
        grad_ref[:, lanes] = grad
        zhat = (columns_of(z_refs, row) - rows[0, row : row + 1, :]) * rows[1, row : row + 1, :]
        before = state_s[row * tall + 7 : row * tall + 7 + frames, :]
        for slot, value in enumerate((grad * zhat, grad, grad * before)):
            held[2 + slot, row : row + 1, :] += jnp.sum(value, axis=0, keepdims=True)

    @pl.when(chunk == 0)
    def _():
        for row in range(blocks):
            at = place_ref[row // per] * per + row % per
            for slot in range(3):
                sums_ref[slot, pl.ds(at, 1), :] = held[2 + slot, row : row + 1, :]


def spots_of_sum(parts, width):
    spots, column = [], 0
    for array, _ in parts:
        spots.append((0, column % (4 * width)))
        column += array.shape[1]
    return spots


def back(layer, place, gate, z, stats, params, ups, states, slopes):
    frames, features = states.shape
    width = features // 4
    blocks = features // LANES
    some = frames // CHUNKS
    whole = lambda array: pl.BlockSpec(array.shape, lambda i: (0,) * array.ndim)

    def by_chunk(array, first=0):
        return pl.BlockSpec(
            (some, array.shape[1]), lambda i: ((first or 0) * CHUNKS + CHUNKS - 1 - i, 0)
        )

    out_shape = [
        jax.ShapeDtypeStruct((frames, features), F32),
        jax.ShapeDtypeStruct((3, blocks, LANES), F32),
    ]
    return call(
        partial(back_body, len(z), len(ups), spots_of_sum(ups, width), layer),
        grid=(CHUNKS,),
        in_specs=[SMEM_SPEC] * 2
        + [by_chunk(a) for a in z]
        + [whole(a) for a in (*stats, params)]
        + [by_chunk(*up) for up in ups]
        + [by_chunk(a) for a in (states, slopes)],
        out_specs=[by_chunk(out_shape[0]), whole(out_shape[1])],
        out_shape=out_shape,
        scratch_shapes=[
            pltpu.VMEM((2, blocks, LANES), F32),
            pltpu.VMEM((blocks, LANES), F32),
            pltpu.VMEM((5, blocks, LANES), F32),
            pltpu.VMEM((blocks * some, LANES), F32),
            pltpu.VMEM((blocks * (some + 8), LANES), F32),
            pltpu.VMEM((blocks * some, LANES), F32),
        ],
        cost_estimate=cost(30 * frames * features, 20 * frames * features),
        name="back",
    )(
        place,
        gate,
        *[in_hbm(a) for a in z],
        *stats,
        params,
        *arrays_of(ups),
        in_hbm(states),
        in_hbm(slopes),
    )


def input_terms(high_s, low_s, weights):
    left, right = [], []
    for block, weight in enumerate(weights):
        w_high, w_low = split(weight)
        left += [high_s[block], low_s[block], high_s[block]]
        right += [w_high, w_high, w_low]
    return dot(jnp.concatenate(left, axis=1), jnp.concatenate(right, axis=0), NN)


def norm_back_body(n_z, split_terms, layer, cols_ref, place_ref, grad_ref, *refs):
    del cols_ref
    z_refs, refs = refs[:n_z], refs[n_z:]
    params_ref, valid_ref, *refs = refs
    stats_refs, sums_refs, weights, refs = refs[:2], refs[2:4], refs[4:14], refs[14:]
    if split_terms:
        out_ref, leave_ref, near_term_ref, far_term_ref, sums_out_ref, *refs = refs
        term_refs, starts = (far_term_ref, near_term_ref), (0, 0)
    else:
        out_ref, leave_ref, term_ref, sums_out_ref, *refs = refs
        term_refs, starts = (term_ref, term_ref), (2 * grad_ref.shape[1] // 4, 0)
    rows, spread, high_s, low_s, far_ref = refs
    blocks = grad_ref.shape[1] // LANES
    width = high_s.shape[2]
    per = width // LANES

    @pl.when(pl.program_id(0) == 0)
    def _():
        count, mean, inv_std = norm_terms(stats_refs)
        to_relative(place_ref, spread, rows, mean, 0)
        to_relative(place_ref, spread, rows, inv_std, 1)
        rows[2] = rows[1] * params_ref[3 * layer]
        sums = [tree(gathered(sums_refs, slot)) for slot in range(3)]
        for slot in range(3):
            sums_out_ref[slot] = sums[slot]
        to_relative(place_ref, spread, rows, sums[0] / count, 3)
        to_relative(place_ref, spread, rows, sums[1] / count, 4)
        valid = valid_ref[...]
        for row in range(blocks):
            lanes = slice(row * LANES, (row + 1) * LANES)
            one = lambda slot: rows[slot, row : row + 1, :]
            zhat = (columns_of(z_refs, row) - one(0)) * one(1)
            value = one(2) * (grad_ref[:, lanes] - valid * (one(4) + zhat * one(3)))
            out_ref[:, lanes] = value
            if (row // per) % 2:
                at = (row // per // 2) * width + (row % per) * LANES
                leave_ref[:, at : at + LANES] = value
            high, low = split(value)
            inner = slice((row % per) * LANES, (row % per + 1) * LANES)
            high_s[row // per, :, inner] = high
            low_s[row // per, :, inner] = low

    value = input_terms(high_s, low_s, weight_blocks(place_ref, weights, far_ref))
    for step, (term_ref, first) in enumerate(zip(term_refs, starts)):

        @pl.when(pl.program_id(0) == step)
        def _():
            for pair in range(2):
                at = pl.multiple_of(((place_ref[0] & 1) ^ pair) * width, width)
                term_ref[:, pl.ds(first + at, width)] = value[
                    :, pair * width : (pair + 1) * width
                ]


def norm_back(columns, place, grad, z, params, valid, stats, sums, weights, layer, split_terms):
    frames, features = grad.shape
    width = features // 4
    blocks = features // LANES
    whole = lambda array: pl.BlockSpec(array.shape, lambda s, cols, place: (0,) * array.ndim)
    operands = [grad, *[in_hbm(a) for a in z], params, valid, *stats, *sums]
    full = jax.ShapeDtypeStruct((frames, features), F32)
    half = jax.ShapeDtypeStruct((frames, 2 * width), F32)
    terms = [half, half] if split_terms else [full]
    out_shape = [full, half, *terms, jax.ShapeDtypeStruct((3, blocks, LANES), F32)]
    return call(
        partial(norm_back_body, len(z), split_terms, layer),
        grid_spec=pltpu.PrefetchScalarGridSpec(
            num_scalar_prefetch=2,
            grid=(2,),
            in_specs=[whole(a) for a in operands] + weight_specs(weights, layer),
            out_specs=[whole(a) for a in out_shape],
            scratch_shapes=[
                pltpu.VMEM((5, blocks, LANES), F32),
                pltpu.VMEM((blocks, LANES), F32),
                pltpu.VMEM((4, frames, width), BF16),
                pltpu.VMEM((4, frames, width), BF16),
                far_scratch(width),
            ],
        ),
        out_shape=out_shape,
        hbm_outs=(0,),
        cost_estimate=cost(6 * frames * features * features, 4 * features * features),
        name="norm_back",
    )(columns, place, *operands, *[in_hbm(w) for w in weights])


def own_terms_body(n_ups, spots, cols_ref, place_ref, grad_ref, *refs):
    del cols_ref
    ups, refs = refs[:n_ups], refs[n_ups:]
    weights, refs = refs[:10], refs[10:]
    out_ref, high_s, low_s, far_ref = refs
    width = high_s.shape[2]
    step = pl.program_id(0)

    @pl.when(step == 0)
    def _():
        for block in range(4):
            high, low = split(grad_ref[:, block * width : (block + 1) * width])
            high_s[block] = high
            low_s[block] = low

    value = input_terms(high_s, low_s, weight_blocks(place_ref, weights, far_ref))
    for pair in range(2):
        at = pl.multiple_of(((place_ref[0] & 1) ^ pair) * width, width)
        out_ref[:, pl.ds(at, width)] = value[:, pair * width : (pair + 1) * width]
    for half in range(2):

        @pl.when(step == half)
        def _():
            first = 2 * half * width
            for (_, column), up in zip(spots, ups):
                low = max(column, first)
                high = min(column + up.shape[1], first + 2 * width)
                if low < high:
                    out_ref[:, low - first : high - first] += up[:, low - column : high - column]


def own_terms(columns, place, grad, ups, weights, layer):
    frames, features = grad.shape
    width = features // 4
    whole = lambda array: pl.BlockSpec(array.shape, lambda s, cols, place: (0,) * array.ndim)
    step_block = pl.BlockSpec((frames, 2 * width), lambda s, cols, place: (0, s))
    return call(
        partial(own_terms_body, len(ups), spots_of_sum(ups, width)),
        grid_spec=pltpu.PrefetchScalarGridSpec(
            num_scalar_prefetch=2,
            grid=(2,),
            in_specs=[whole(grad)]
            + [part_spec(up, frames) for up in ups]
            + weight_specs(weights, layer),
            out_specs=step_block,
            scratch_shapes=[pltpu.VMEM((4, frames, width), BF16)] * 2 + [far_scratch(width)],
        ),
        out_shape=jax.ShapeDtypeStruct((frames, features), F32),
        cost_estimate=cost(6 * frames * features * features, 4 * features * features),
        name="own_terms",
    )(columns, place, in_hbm(grad), *arrays_of(ups), *[in_hbm(w) for w in weights])


def prepare_body(n_chunks, lists_ref, place_ref, *refs):
    del lists_ref
    groups = []
    for _ in range(4):
        groups.append(refs[:n_chunks])
        refs = refs[n_chunks:]
    high_ref, low_ref = refs
    padded = high_ref.shape[0] // 2
    width = high_ref.shape[1] // 2
    for side in range(2):

        @pl.when(pl.program_id(0) // 2 == side)
        def _():
            for clip in range(2):
                for dc in range(2):
                    at = pl.multiple_of((place_ref[6] ^ clip ^ dc) * width, width)
                    row = clip * padded
                    for part in groups[2 * clip + side]:
                        rows = part.shape[0]
                        high, low = split(part[:, dc * width : (dc + 1) * width])
                        high_ref[row : row + rows, pl.ds(at, width)] = high
                        low_ref[row : row + rows, pl.ds(at, width)] = low
                        row += rows
                rest = (clip + 1) * padded - row
                zeros = jnp.zeros((rest, 2 * width), BF16)
                high_ref[row : row + rest, :] = zeros
                low_ref[row : row + rest, :] = zeros


def prepare(lists, place, groups):
    width = groups[0][0].shape[1] // 4
    frames = sum(part.shape[0] for part in groups[0])
    padded = -(-frames // LANES) * LANES
    in_specs = []
    for i, group in enumerate(groups):
        for part in group:
            if i % 2 == 0:
                index = lambda s, *_: (0, jnp.minimum(s, 1))
            else:
                index = lambda s, *_: (0, jnp.maximum(s - 2, 0))
            in_specs.append(pl.BlockSpec((part.shape[0], 2 * width), index))
    out = jax.ShapeDtypeStruct((2 * padded, 8 * width), BF16)
    out_spec = pl.BlockSpec((2 * padded, 2 * width), lambda s, cols, place: (0, cols[s]))
    return call(
        partial(prepare_body, len(groups[0])),
        grid_spec=pltpu.PrefetchScalarGridSpec(
            num_scalar_prefetch=2,
            grid=(4,),
            in_specs=in_specs,
            out_specs=[out_spec, out_spec],
        ),
        out_shape=[out, out],
        hbm_outs=(0, 1),
        cost_estimate=cost(0, 16 * frames * 8 * width),
        name="prepare",
    )(lists, place, *[in_hbm(part) for group in groups for part in group])


def product(g_high, g_low, x_high, x_low):
    return dot(g_high, x_high, NN) + (dot(g_high, x_low, NN) + dot(g_low, x_high, NN))


def weight_body(turn, place_ref, *refs):
    if turn:
        grad_ref, near_ref, x_high, x_low, kept, sent, g_high, g_low, t_high, t_low = refs

        @pl.when(pl.program_id(0) == 0)
        def _():
            frames, features = grad_ref.shape
            width = features // 4
            rows = width // 4
            padded = t_high.shape[1] // 2
            t_high[...] = jnp.zeros_like(t_high)
            t_low[...] = jnp.zeros_like(t_low)
            for clip in range(2):
                for dh in range(2):
                    if clip == 0:
                        part = grad_ref[:, 2 * dh * width : (2 * dh + 1) * width]
                    else:
                        part = near_ref[:, dh * width : (dh + 1) * width]
                    high, low = split(part.T)
                    at = (
                        slice(dh * width, (dh + 1) * width),
                        slice(clip * padded, clip * padded + frames),
                    )
                    t_high[at] = high
                    t_low[at] = low
            for group in range(8):
                first, second, dh = group // 4, group // 2 % 2, group % 2
                core = place_ref[6]
                y = place_ref[4] ^ (first * core + second * (1 - core))
                x = place_ref[5] ^ (first * (1 - core) + second * core)
                at = pl.multiple_of(dh * width + (2 * y + x) * rows, rows)
                g_high[group * rows : (group + 1) * rows, :] = t_high[pl.ds(at, rows), :]
                g_low[group * rows : (group + 1) * rows, :] = t_low[pl.ds(at, rows), :]

    else:
        g_high, g_low, x_high, x_low, kept, sent = refs
    half = g_high.shape[0] // 2
    value = product(g_high[...], g_low[...], x_high[...], x_low[...])
    kept[...] = value[:half].reshape(kept.shape)
    sent[...] = value[half:].reshape(sent.shape)


def weight_rows(half, place, grads, x_split, width):
    turn = half == 0
    whole = lambda array: pl.BlockSpec(array.shape, lambda s, place: (0,) * array.ndim)
    x_spec = pl.BlockSpec((x_split[0].shape[0], width), lambda s, place: (0, 4 * half + s))
    shape = (2, 2, width // 4, 4 * width)
    out_shape = [jax.ShapeDtypeStruct(shape, F32)] * 2
    out_specs = [pl.BlockSpec(shape[:3] + (width,), lambda s, place: (0, 0, 0, s))] * 2
    scratch = []
    if turn:
        turned = (2 * width, x_split[0].shape[0])
        out_shape += [jax.ShapeDtypeStruct(turned, BF16)] * 2
        out_specs += [whole(out_shape[-1])] * 2
        scratch = [pltpu.VMEM(turned, BF16)] * 2
    return call(
        partial(weight_body, turn),
        grid_spec=pltpu.PrefetchScalarGridSpec(
            num_scalar_prefetch=1,
            grid=(4,),
            in_specs=[whole(a) for a in grads] + [x_spec] * 2,
            out_specs=out_specs,
            scratch_shapes=scratch,
        ),
        out_shape=out_shape,
        hbm_outs=(0,),
        cost_estimate=cost(12 * x_split[0].shape[0] * width * 4 * width, 4 * 8 * width * width),
        name="weight_rows",
    )(place, *([in_hbm(grads[0]), grads[1]] if turn else grads), *[in_hbm(x) for x in x_split])


def step_body(n, widths, cut, *refs):
    ins, outs = refs[: 2 * n], refs[2 * n :]
    starts = [sum(widths[:i]) for i in range(len(widths))]
    column = 0
    for i in range(n):
        total = ins[2 * i][...] + ins[2 * i + 1][...]
        end = column + total.shape[-1]
        for j, (start, columns) in enumerate(zip(starts, widths)):
            low, high = max(start, column), min(start + columns, end)
            if low < high:
                to = (Ellipsis, slice(low - start, high - start))
                piece = total[..., low - column : high - column]
                if cut:
                    outs[2 * j][to] = piece[0]
                    outs[2 * j + 1][to] = piece[1]
                else:
                    outs[j][to] = piece
        column = end


def step_of(*pairs, cut=True, widths=None):
    shape = list(pairs[0][0].shape)
    widths = widths or [sum(pair[0].shape[-1] for pair in pairs)]
    outs = []
    for columns in widths:
        shape[-1] = columns
        out = jax.ShapeDtypeStruct(tuple(shape[1:] if cut else shape), F32)
        outs += [out] * (1 + cut)
    whole = lambda array: pl.BlockSpec(array.shape, lambda i: (0,) * array.ndim)
    operands = [array for pair in pairs for array in pair]
    return call(
        partial(step_body, len(pairs), widths, cut),
        grid=(1,),
        in_specs=[whole(a) for a in operands],
        out_specs=[whole(a) for a in outs],
        out_shape=outs,
        cost_estimate=cost(0, 4 * sum(a.size for a in operands)),
        name="reduction_step",
    )(*operands)


def plane_swap(array, step):
    pairs = []
    for i in range(8):
        over_x = (i % 2 == 0) == (step == 0)
        pairs.append((i, i ^ 2 if over_x else i ^ 4))
    return lax.ppermute(array, ("y", "x", "c"), pairs)


def plane_gather(share, *before):
    first = plane_swap(share, 0)
    second = plane_swap(share, 1)
    return [share, second, first, plane_swap(after(first, *before), 1)]


def assemble_body(groups, place_ref, *refs):
    out_ref = refs[-1]
    core = place_ref[6]
    column = 0
    for group in range(groups):
        rows, columns = refs[4 * group].shape
        for i in range(4):
            first, second = i // 2, i % 2
            y = place_ref[4] ^ (first * core + second * (1 - core))
            x = place_ref[5] ^ (first * (1 - core) + second * core)
            at = pl.multiple_of((2 * y + x) * rows, rows)
            out_ref[0, pl.ds(at, rows), column : column + columns] = refs[4 * group + i][...]
        column += columns


def assemble(place, groups, layer, onto=None):
    pieces = [piece for group in groups for piece in group]
    rows = 4 * pieces[0].shape[0]
    columns = sum(group[0].shape[1] for group in groups)
    aliases, extra, extra_specs = {}, [], []
    if onto is not None:
        aliases, extra = {1 + len(pieces): 0}, [onto]
        extra_specs = [pl.BlockSpec(memory_space=pl.ANY)]
    (out,) = call(
        partial(assemble_body, len(groups)),
        grid=(1,),
        out_shape=[jax.ShapeDtypeStruct((LAYERS, rows, columns), F32)],
        hbm_outs=(0,),
        in_specs=[SMEM_SPEC]
        + [pl.BlockSpec(p.shape, lambda i: (0, 0)) for p in pieces]
        + extra_specs,
        out_specs=[pl.BlockSpec((1, rows, columns), lambda i: (layer, 0, 0))],
        input_output_aliases=aliases,
        cost_estimate=cost(0, 8 * rows * columns),
        name="assemble",
    )(place, *[p if extra else in_hbm(p) for p in pieces], *extra)
    return out


def half_features(inputs, weights, gains, shifts, decays, biases, lengths, frame_mask, grad_out):
    width, slots = inputs.shape
    clips, frames = frame_mask.shape
    depth = weights.shape[2]
    blocks = 4 * width // LANES
    y, x, h, l, c = (lax.axis_index(name) for name in ("y", "x", "h", "l", "c"))
    b = 2 * y + x
    numbers = [2 * (h ^ (rel // 2)) + (c ^ (rel % 2)) for rel in range(4)] + [y, x, c]
    place = jnp.stack(numbers).astype(jnp.int32)
    own_blocks, other_blocks = (
        jnp.stack(
            [2 * (2 * (h ^ (rel // 2)) + half) + (c ^ (rel % 2)) for rel in range(4)]
        ).astype(jnp.int32)
        for half in (l, 1 - l)
    )
    own_columns = jnp.stack([2 * h + l, 2 * (1 - h) + l]).astype(jnp.int32)
    other_columns = jnp.stack([2 * (1 - h) + 1 - l, 2 * h + 1 - l]).astype(jnp.int32)
    all_columns = jnp.concatenate([own_columns, other_columns[::-1]])
    rows = width // 4

    clip = 2 * h + c
    seen = lax.dynamic_index_in_dim(frame_mask, clip, 0, keepdims=False)
    length = lax.dynamic_index_in_dim(lengths, clip, 0, keepdims=False)
    moments = jnp.arange(frames, dtype=jnp.int32)
    gate = ((moments < length) & ((seen == 1) | (moments == 0))).astype(F32)
    valid = jnp.broadcast_to(gate[:, None], (frames, LANES))

    def far_share(layer):
        return lax.dynamic_slice(weights, (layer, b * rows, 0), (1, rows, depth))[0]

    def over_h(array):
        return lax.ppermute(array, "h", FLIP2)

    def over_c(array):
        return lax.ppermute(array, "c", FLIP2)

    def over_second(array):
        return plane_swap(array, 1)

    def four_of(near_rows, far_rows):
        return [
            (near_rows, 0),
            (over_c(near_rows), 1),
            (far_rows, 0),
            (over_c(far_rows), 1),
        ]

    def far_pieces(share):
        both = lax.ppermute(share, ("y", "x"), DIAGONAL)
        return [share, lax.ppermute(share, "x", FLIP2), lax.ppermute(share, "y", FLIP2), both]

    near = over_c(weights)
    share = far_share(0)
    close, away = pack(place, after(inputs, share), frames)
    share = over_h(share)
    away = over_h(away)
    other_close = swap_half(close)
    up_close, up_away = pack(place, after(grad_out, close), frames, waits=True)
    share = after(share, up_close, valid, near, other_close)
    pieces = far_pieces(share)
    away = after(away, pieces[1:])
    half_weights = [[weights, near, *pieces, *map(over_c, after(pieces, away))]]
    own = four_of(after(close, away), away)
    others = four_of(other_close, swap_half(away))
    params = jnp.stack([gains, shifts + biases, decays], axis=1)
    own_params = params.reshape(LAYERS * 3 * width // LANES, LANES)
    params = None

    def gather(array):
        mine = lax.all_gather(array, ("y", "x", "h"), tiled=True)
        return [mine, over_c(mine)]

    weight = half_weights[0]
    early = jnp.concatenate([own_blocks, other_blocks[:2]])
    z, own_flat = project(place, frames, own + others[:2], early, weight, 0, flat=own)
    z, stats, other_flat = project(
        place,
        frames,
        others[2:],
        other_blocks[2:],
        weight,
        0,
        z,
        valid,
        params=own_params,
        flat=others,
    )
    z = [z]
    stats = gather(stats)
    share = over_c(lax.ppermute(after(far_share(1), stats[0]), ("h", "c"), DIAGONAL))
    x, states, slopes, params = recur(0, place, gate, z, stats, None, valid, own_flat, False)
    groups = [[own_flat], [other_flat]]
    groups += [[over_c(after(p, z[0])) for p in group] for group in groups]
    x_split = prepare(all_columns, place, after(groups, slopes))
    saved = [(groups, x_split, z, stats, states, slopes)]

    up_away = over_h(after(up_away, share))
    pieces = far_pieces(after(share, slopes, groups))
    near = [weights, near]
    other = swap_half(x)
    z, *_ = project(place, frames, [(x, None)], own_blocks, near, 1)
    far = [*pieces, *map(over_c, after(pieces, z))]
    half_weights.append(near + far)
    z, stats = project(place, frames, [(other, None)], other_blocks, near, 1, z, valid)
    both = jnp.concatenate([own_blocks, other_blocks])
    z_far, stats = project(
        place,
        frames,
        [(x, None), (other, None)],
        both,
        far,
        1,
        None,
        valid,
        stats,
    )
    z = [z, z_far]
    upstream = four_of(up_close, after(up_away, z_far))
    stats = gather(stats)
    *output, states, slopes = recur(1, place, gate, z, stats, params, valid, x, True)
    groups = [[x], [other]]
    groups += [[over_c(after(p, slopes)) for p in group] for group in groups]
    saved.append((groups, None, z, stats, states, slopes))
    diagonal = over_c(over_h(output[3]))

    ups = upstream
    results = [None] * LAYERS
    for layer in range(LAYERS - 1, -1, -1):
        groups, x_split, z, stats, states, slopes = saved[layer]
        weight = half_weights[layer]
        grad_pre, sums = back(layer, place, gate, z, stats, params, ups, states, slopes)
        sums = gather(sums)
        if layer == 0:
            later, go = step_of(*[(in_hbm(k), after(g, sums[0])) for k, g in zip(stay, come)])
            sums = after(sums, later)
            go = over_second(go)
        else:
            away = over_h(after(output[2], sums[0]))
        grad_z, leaving, *terms, sums = norm_back(
            other_columns, place, grad_pre, z, params, valid, stats, sums, weight, layer,
            layer == 0,
        )
        leaving = over_c(leaving)
        if layer > 0:
            received = [swap_half(terms[0])]
            x_split = prepare(all_columns, place, after(groups, grad_z, diagonal))
        else:
            received = [None, swap_half(terms[1])]
            later, go = step_of((later, after(go, grad_z)))
            leaving = after(leaving, later)
            later = (later, over_h(go))
        *first, g_high, g_low = weight_rows(0, place, (grad_z, leaving), x_split, width)
        turned = (g_high, g_low)
        come = [plane_swap(first[1], 0)]
        if layer > 0:
            turned = after(turned, away)
            output = [(a, 0) for a in (output[0], over_c(output[1]), away, diagonal)]
        else:
            received[0] = swap_half(after(terms[0], received[1]))
        second = weight_rows(1, place, turned, x_split, width)
        come.append(plane_swap(second[1], 0))
        stay = (first[0], second[0])
        kept = own_terms(own_columns, place, after(grad_z, second[0]), ups, weight, layer)
        ups = [(kept, None)] + [(r, None) for r in received]
        results[layer] = lax.dynamic_index_in_dim(
            sums.reshape(3, 4, width), clip, axis=1, keepdims=False
        )

    away = merge(kept, 1, received[1])
    (later,) = step_of((later[0], after(later[1], away)), cut=False)
    away = over_h(away)
    later_first, later_second = plane_swap(later, 0), plane_swap(later, 1)
    total, go = step_of((in_hbm(stay[0]), after(come[0], later_first)), (in_hbm(stay[1]), come[1]))
    go = over_second(go)
    later = [later, later_second, later_first, plane_swap(after(later_first, total), 1)]
    far = [(away, 0), (over_c(away), 1)]
    total, go = step_of((total, after(go, far[1][0])))
    go = over_h(go)
    output = unpack(place, [(after(array, total), i) for array, i in output], frames, waited=True)
    grad_weights = assemble(place, after([later], output), 1)
    (share,) = step_of((total, after(go, grad_weights)), cut=False)
    gathered = plane_gather(share)
    close = merge(kept, 0, after(received[0], gathered[2]))
    grad_in = [(close, 0), (over_c(close[frames:]), 0)] + far
    grad_in = unpack(place, grad_in, frames)
    grad_weights = assemble(place, after([gathered], grad_in), 0, grad_weights)
    sums = jnp.stack(results)
    return (
        output,
        grad_in,
        grad_weights,
        sums[:, 0],
        sums[:, 1],
        sums[:, 2],
        sums[:, 1],
    )


def gelu_slope(value):
    return (
        0.5 * (1.0 + jax.scipy.special.erf(value / ROOT_TWO))
        + value * jnp.exp(-0.5 * value * value) / ROOT_TWO_PI
    )


def recur_step(decay, state, inputs):
    drive_t, valid_t = inputs
    pre = drive_t + decay * state
    state = state + valid_t * (jax.nn.gelu(pre, approximate=False) - state)
    return (state, state)


def back_step(decay, carry, inputs):
    upstream_t, valid_t, pre_t = inputs
    total = upstream_t + carry
    grad_pre = total * valid_t * gelu_slope(pre_t)
    carry = total * (1.0 - valid_t) + grad_pre * decay
    return (carry, grad_pre)


def add_piece(weight, piece):
    return jnp.dot(weight, piece, precision=HIGH, preferred_element_type=jnp.float32)


def weight_columns(grad_pre_norm, piece):
    return jnp.einsum("jf,kf->jk", grad_pre_norm, piece, precision=HIGH)


def split_features(inputs, weights, gains, shifts, decays, biases, lengths, frame_mask, grad_out):
    width, slots = inputs.shape
    clips, frames_len = frame_mask.shape
    frames = jnp.arange(frames_len, dtype=jnp.int32)
    valid_grid = (
        (frames[None, :] < lengths[:, None]) & ((frame_mask == 1) | (frames[None, :] == 0))
    ).astype(jnp.float32)
    valid = valid_grid.reshape(-1)
    valid_row = valid[None, :]
    valid_time = jnp.broadcast_to(valid_grid.T[:, :, None], (frames_len, clips, width)).reshape(
        frames_len, clips * width
    )
    count_local = jnp.sum(valid)

    def to_time(array):
        return jnp.transpose(array.reshape(width, clips, frames_len), (2, 1, 0)).reshape(
            frames_len, clips * width
        )

    def from_time(array):
        return jnp.transpose(array.reshape(frames_len, clips, width), (2, 1, 0)).reshape(
            width, slots
        )

    layer_in = inputs
    saved = []
    for layer_no in range(LAYERS):
        weight = weights[layer_no]
        gathered = lax.all_gather(layer_in, "neuron", axis=0, tiled=True)
        pre_norm = add_piece(weight, gathered)
        first_sum, count = lax.psum((jnp.sum(valid_row * pre_norm, axis=1), count_local), "batch")
        mean = first_sum / count
        centered = pre_norm - mean[:, None]
        var = lax.psum(jnp.sum(valid_row * centered * centered, axis=1), "batch") / count
        inv_std = lax.rsqrt(var + EPS)
        zhat = (pre_norm - mean[:, None]) * inv_std[:, None]
        drive = gains[layer_no][:, None] * zhat + (shifts[layer_no] + biases[layer_no])[:, None]
        drive_time = to_time(drive)
        decay_wide = jnp.tile(decays[layer_no], clips)
        start_state = jnp.zeros((clips * width,), jnp.float32)
        _, states = lax.scan(
            partial(recur_step, decay_wide), start_state, (drive_time, valid_time), unroll=8
        )
        saved.append((gathered, zhat, inv_std, drive_time, states, count))
        layer_in = layer_in + valid_row * from_time(states)
    upstream = grad_out
    grad_parts = [None] * LAYERS
    for layer_no in range(LAYERS - 1, -1, -1):
        gathered, zhat, inv_std, drive_time, states, count = saved[layer_no]
        decay_wide = jnp.tile(decays[layer_no], clips)
        gain = gains[layer_no]
        previous = jnp.concatenate([jnp.zeros_like(states[:1]), states[:-1]], axis=0)
        pre_time = drive_time + decay_wide[None, :] * previous
        grad_state = to_time(valid_row * upstream)
        start_carry = jnp.zeros((clips * width,), jnp.float32)
        _, grad_pre_time = lax.scan(
            partial(back_step, decay_wide),
            start_carry,
            (grad_state, valid_time, pre_time),
            reverse=True,
            unroll=8,
        )
        decay_local = jnp.sum(
            jnp.sum(grad_pre_time * previous, axis=0).reshape(clips, width), axis=0
        )
        grad_pre = from_time(grad_pre_time)
        gain_local = jnp.sum(grad_pre * zhat, axis=1)
        shift_local = jnp.sum(grad_pre, axis=1)
        grad_gain, grad_shift, grad_decay = lax.psum(
            (gain_local, shift_local, decay_local), "batch"
        )
        grad_pre_norm = (gain * inv_std)[:, None] * (
            grad_pre - valid_row * (grad_shift[:, None] + zhat * grad_gain[:, None]) / count
        )
        weight_local = weight_columns(grad_pre_norm, gathered)
        input_terms = jnp.einsum("jk,jf->kf", weights[layer_no], grad_pre_norm, precision=HIGH)
        input_grad = lax.psum_scatter(input_terms, "neuron", scatter_dimension=0, tiled=True)
        grad_weight = lax.psum(weight_local, "batch")
        upstream = upstream + input_grad
        grad_parts[layer_no] = (grad_weight, grad_gain, grad_shift, grad_decay)
    grad_weights = jnp.stack([grad_parts[layer_no][0] for layer_no in range(LAYERS)])
    grad_gains = jnp.stack([grad_parts[layer_no][1] for layer_no in range(LAYERS)])
    grad_shifts = jnp.stack([grad_parts[layer_no][2] for layer_no in range(LAYERS)])
    grad_decays = jnp.stack([grad_parts[layer_no][3] for layer_no in range(LAYERS)])
    return (layer_in, upstream, grad_weights, grad_gains, grad_shifts, grad_decays, grad_shifts)


def solution(mesh):
    if (mesh.shape["batch"], mesh.shape["neuron"]) == (4, 8):
        cut = Mesh(mesh.devices.reshape(2, 2, 2, 2, 2), ("y", "x", "h", "l", "c"))
        batch, neuron, body = ("y", "x"), ("h", "l", "c"), half_features
    else:
        cut, batch, neuron, body = mesh, "batch", "neuron", split_features
    in_specs = (
        P(neuron, batch),
        P(None, neuron, None),
        P(None, neuron),
        P(None, neuron),
        P(None, neuron),
        P(None, neuron),
        P(batch),
        P(batch, None),
        P(neuron, batch),
    )
    out_specs = (
        P(neuron, batch),
        P(neuron, batch),
        P(None, neuron, None),
        P(None, neuron),
        P(None, neuron),
        P(None, neuron),
        P(None, neuron),
    )
    return jax.shard_map(
        body, mesh=cut, in_specs=in_specs, out_specs=out_specs, check_vma=False
    )
```

```python
from functools import partial
import math

import jax
import jax.numpy as jnp
from jax import lax
from jax.experimental import pallas as pl
from jax.experimental.pallas import tpu as pltpu
from jax.sharding import Mesh, PartitionSpec as P

LAYERS = 2
EPS = 1e-05
HIGH = lax.Precision.HIGHEST
ROOT_TWO = math.sqrt(2.0)
ROOT_TWO_PI = math.sqrt(2.0 * math.pi)
F32 = jnp.float32
BF16 = jnp.bfloat16
LANES = 128
VMEM_LIMIT = 24 * 1024 * 1024
SMEM_SPEC = pl.BlockSpec(memory_space=pltpu.SMEM)
VMEM_SPEC = pl.BlockSpec(memory_space=pltpu.VMEM)


FLIP2 = [(0, 1), (1, 0)]
DIAGONAL = [(0, 3), (1, 2), (2, 1), (3, 0)]


def swap_half(array):
    return lax.ppermute(array, "l", FLIP2)


def after(value, *others):
    return lax.optimization_barrier((value, others))[0]


def split(value):
    high = value.astype(BF16)
    return high, (value - high.astype(F32)).astype(BF16)


def dot(a, b, dims):
    return lax.dot_general(a, b, (dims, ((), ())), preferred_element_type=F32)


NT = ((1,), (1,))
NN = ((1,), (0,))


def in_hbm(array):
    return pltpu.with_memory_space_constraint(array, pltpu.HBM)


def call(body, out_shape, hbm_outs=(), **kwargs):
    if hbm_outs:
        out_shape = [
            pltpu.HBM(a.shape, a.dtype) if i in hbm_outs else a for i, a in enumerate(out_shape)
        ]
    return pl.pallas_call(
        body,
        out_shape=out_shape,
        compiler_params=pltpu.CompilerParams(vmem_limit_bytes=VMEM_LIMIT),
        **kwargs,
    )


def cost(flops, byte_count):
    return pl.CostEstimate(flops=int(flops) // 64, bytes_accessed=int(byte_count) // 64, transcendentals=0)


def pack_body(frames, place_ref, in_ref, near_ref, far_ref, turned):
    slots = in_ref.shape[1]
    for start in range(0, slots, LANES):
        turned[start : start + LANES, :] = in_ref[:, start : start + LANES].T
    for rel in range(4):
        first = pl.multiple_of(place_ref[rel] * frames, 8)
        out = (near_ref, far_ref)[rel // 2]
        out[(rel % 2) * frames : (rel % 2 + 1) * frames, :] = turned[pl.ds(first, frames), :]


def pack(place, array, frames, waits=False):
    width, slots = array.shape
    out = jax.ShapeDtypeStruct((2 * frames, width), F32)
    return call(
        partial(pack_body, frames),
        grid=(1,),
        out_shape=[out, out],
        in_specs=[SMEM_SPEC, pl.BlockSpec((width, slots), lambda i: (0, 0))],
        out_specs=[pl.BlockSpec(out.shape, lambda i: (0, 0))] * 2,
        scratch_shapes=[pltpu.VMEM((slots, width), F32)],
        hbm_outs=(0, 1) if waits else (),
        cost_estimate=cost(0, 8 * width * slots),
        name="pack",
    )(place, in_hbm(array))


def part_spec(part, frames):
    array, i = part
    if i is None:
        return pl.BlockSpec(array.shape, lambda *_: (0,) * array.ndim)
    return pl.BlockSpec((frames, array.shape[1]), lambda *_: (i, 0))


def arrays_of(parts):
    return [array for array, _ in parts]


def unpack_body(frames, place_ref, *refs):
    ins, out_ref, turned = refs[:4], refs[4], refs[5]
    slots = out_ref.shape[1]
    for rel in range(4):
        first = pl.multiple_of(place_ref[rel] * frames, 8)
        turned[pl.ds(first, frames), :] = ins[rel][...]
    for start in range(0, slots, LANES):
        out_ref[:, start : start + LANES] = turned[start : start + LANES, :].T


def unpack(place, parts, frames, waited=False):
    width = parts[0][0].shape[1]
    slots = 4 * frames
    return call(
        partial(unpack_body, frames),
        grid=(1,),
        out_shape=jax.ShapeDtypeStruct((width, slots), F32),
        in_specs=[SMEM_SPEC] + [part_spec(part, frames) for part in parts],
        out_specs=pl.BlockSpec((width, slots), lambda i: (0, 0)),
        scratch_shapes=[pltpu.VMEM((slots, width), F32)],
        cost_estimate=cost(0, 8 * width * slots),
        name="unpack",
    )(place, *[in_hbm(a) if waited else a for a in arrays_of(parts)])


def merge_body(kept_ref, come_ref, out_ref):
    frames, columns = kept_ref.shape
    width = columns // 2
    for i in range(2):
        some = slice(i * width, (i + 1) * width)
        out_ref[i * frames : (i + 1) * frames, :] = kept_ref[:, some] + come_ref[:, some]


def merge(kept, half, come):
    frames, columns = come.shape
    return call(
        merge_body,
        grid=(1,),
        out_shape=jax.ShapeDtypeStruct((2 * frames, columns // 2), F32),
        in_specs=[
            pl.BlockSpec((frames, columns), lambda i: (0, half)),
            pl.BlockSpec((frames, columns), lambda i: (0, 0)),
        ],
        out_specs=pl.BlockSpec((2 * frames, columns // 2), lambda i: (0, 0)),
        cost_estimate=cost(0, 12 * frames * columns),
        name="merge",
    )(kept, come)


def project_body(n_parts, n_flat, spots, n_weights, first, with_acc, with_stats, with_params, cols_ref, place_ref, *refs):
    del cols_ref

    def take(n):
        nonlocal refs
        some, refs = refs[:n], refs[n:]
        return some

    parts, flat_parts, weights = take(n_parts), take(n_flat), take(n_weights)
    acc, valid, stats_in, params = take(with_acc), take(with_stats > 0), take(with_stats > 1), take(with_params)
    (out_ref,) = take(1)
    stats, flat = take(with_stats > 0), take(n_flat > 0)
    x_high, x_low, far_ref = refs
    step = pl.program_id(0)
    width = x_high.shape[2]

    @pl.when(step == 0)
    def _():
        for block, part in zip(spots, parts):
            for start in range(0, part.shape[1], width):
                high, low = split(part[:, start : start + width])
                x_high[block + start // width] = high
                x_low[block + start // width] = low
        column = 0
        for part in flat_parts:
            flat[0][:, column : column + part.shape[1]] = part[...]
            column += part.shape[1]
        if with_acc:
            out_ref[...] = acc[0][...]
        else:
            out_ref[...] = jnp.zeros_like(out_ref)

    stacked = jnp.concatenate([x_high[step], x_low[step], x_high[step]], axis=1)
    for block, weight in enumerate(weight_blocks(place_ref, weights, far_ref)):
        w_high, w_low = split(weight)
        columns = slice(block * width, (block + 1) * width)
        out_ref[:, columns] += dot(stacked, jnp.concatenate([w_high, w_high, w_low], axis=1), NT)

    if with_stats:
        (stats_ref,) = stats

        @pl.when(step == pl.num_programs(0) - 1)
        def _():
            if stats_in:
                stats_ref[...] = stats_in[0][...]
            own = jnp.sum(valid[0][...], axis=0, keepdims=True)
            per = width // LANES
            for row in range(out_ref.shape[1] // LANES):
                z = out_ref[:, row * LANES : (row + 1) * LANES]
                total = jnp.sum(valid[0][...] * z, axis=0, keepdims=True)
                centred = valid[0][...] * (z - total / own)
                squares = jnp.sum(centred * centred, axis=0, keepdims=True)
                at = place_ref[first + row // per] * per + row % per
                stats_ref[0, pl.ds(at, 1), :] = total
                stats_ref[1, pl.ds(at, 1), :] = squares
                stats_ref[2, pl.ds(at, 1), :] = own
            if with_params:
                rest = params[0].shape[0] - 8
                stats_ref[3] = params[0][:8, :]
                stats_ref[4] = jnp.zeros_like(stats_ref[4])
                stats_ref[4, :rest, :] = params[0][8:, :]


def weight_specs(weights, layer, pairs=2):
    specs = []
    for weight in weights:
        if weight.ndim == 3:
            shape = (1, weight.shape[1], pairs * weight.shape[1])
            specs.append(pl.BlockSpec(shape, lambda s, cols, *_: (layer, 0, cols[s])))
        else:
            shape = (weight.shape[0], pairs * 4 * weight.shape[0])
            specs.append(pl.BlockSpec(shape, lambda s, cols, *_: (0, cols[s])))
    return specs


def far_scratch(width, pairs=2):
    return pltpu.VMEM((2, width, pairs * width), F32)


def weight_blocks(place_ref, refs, far_ref):
    near = [ref[0] for ref in refs if len(ref.shape) == 3]
    pieces = [ref for ref in refs if len(ref.shape) == 2]
    far = []
    for i in range(len(pieces) // 4):
        for rel, piece in enumerate(pieces[4 * i : 4 * i + 4]):
            rows = piece.shape[0]
            row = 2 * (place_ref[4] ^ (rel // 2)) + (place_ref[5] ^ (rel % 2))
            far_ref[i, pl.ds(pl.multiple_of(row * rows, rows), rows), :] = piece[...]
        far.append(far_ref[i])
    return near + far


def project(
    place, frames, parts, blocks, weights, layer, acc=None, valid=None, stats=None, params=None, flat=()
):
    near = weights[0].ndim == 3
    units = sum(1 if w.ndim == 3 else 0.25 for w in weights)
    width = weights[0].shape[1] if near else 4 * weights[0].shape[0]
    n = blocks.shape[0]
    spots, block = [], 0
    for array, _ in parts:
        spots.append(block)
        block += array.shape[1] // width
    full = pl.BlockSpec(memory_space=pltpu.VMEM)
    in_specs = [part_spec(part, frames) for part in (*parts, *flat)]
    in_specs += weight_specs(weights, layer, 1)
    operands = arrays_of(parts) + arrays_of(flat) + [in_hbm(w) for w in weights]
    array = jax.ShapeDtypeStruct((frames, int(units) * width), F32)
    array_spec = pl.BlockSpec(array.shape, lambda s, cols, place: (0, 0))
    out_shape, out_specs = [array], [array_spec]
    if acc is not None:
        in_specs.append(array_spec)
        operands.append(in_hbm(acc))
    if valid is not None:
        in_specs.append(full)
        operands.append(valid)
        shape = (3 if params is None else 5, 4 * width // LANES, LANES)
        out_shape.append(jax.ShapeDtypeStruct(shape, F32))
        out_specs.append(pl.BlockSpec(shape, lambda s, cols, place: (0, 0, 0)))
    for extra in (stats, params):
        if extra is not None:
            in_specs.append(full)
            operands.append(extra)
    if flat:
        out_shape.append(jax.ShapeDtypeStruct((frames, 4 * width), F32))
        out_specs.append(pl.BlockSpec((frames, 4 * width), lambda s, cols, place: (0, 0)))
    return call(
        partial(
            project_body,
            len(parts),
            len(flat),
            spots,
            len(weights),
            0 if near else 2,
            acc is not None,
            (valid is not None) + (stats is not None),
            params is not None,
        ),
        grid_spec=pltpu.PrefetchScalarGridSpec(
            num_scalar_prefetch=2,
            grid=(n,),
            in_specs=in_specs,
            out_specs=out_specs,
            scratch_shapes=[pltpu.VMEM((n, frames, width), BF16)] * 2 + [far_scratch(width, 1)],
        ),
        out_shape=out_shape,
        hbm_outs=(0, len(out_shape) - 1) if flat else (0,),
        cost_estimate=cost(6 * frames * n * width * units * width, 4 * n * width * units * width),
        name="project",
    )(blocks, place, *operands)


def to_relative(place_ref, spread, rows_ref, value, slot):
    per = value.shape[0] // 4
    spread[...] = value
    for rel in range(4):
        first = place_ref[rel] * per
        for row in range(per):
            rows_ref[slot, rel * per + row : rel * per + row + 1, :] = spread[
                pl.ds(first + row, 1), :
            ]


def tree(values):
    while len(values) > 1:
        values = [a + b for a, b in zip(values[::2], values[1::2])]
    return values[0]


def gathered(ref, slot):
    return [ref[i] for i in range(slot, ref.shape[0], ref.shape[0] // 16)]


def norm_terms(stats_ref):
    each = [gathered(stats_ref, slot) for slot in range(3)]
    totals, squares, owns = each
    count = tree(owns)
    mean = tree(totals) / count
    away = [total / own - mean for total, own in zip(totals, owns)]
    spread = tree([s + n * a * a for s, n, a in zip(squares, owns, away)])
    return count, mean, lax.rsqrt(spread / count + EPS)


CHUNKS = 4


def columns_of(refs, row):
    for ref in refs:
        if row * LANES < ref.shape[1]:
            return ref[:, row * LANES : (row + 1) * LANES]
        row -= ref.shape[1] // LANES


def recur_body(n_z, last, layer, spread_params, place_ref, gate_ref, *refs):
    z_refs, refs = refs[:n_z], refs[n_z:]
    (stats_ref, params_ref, valid_ref, x_ref), refs = refs[:4], refs[4:]
    outs, refs = refs[: 1 + 3 * last], refs[1 + 3 * last :]
    if spread_params:
        state_ref, slope_ref, params_out, rows, spread, held, drive_s, state_s, slope_s = refs
    else:
        state_ref, slope_ref, rows, spread, held, drive_s, state_s, slope_s = refs
    frames, features = x_ref.shape
    blocks = features // LANES
    per = blocks // 4
    chunk = pl.program_id(0)

    @pl.when(chunk == 0)
    def _():
        if spread_params:
            for rel in range(4):
                first = place_ref[rel] * (stats_ref.shape[0] // 16) + 3
                for row in range(LAYERS * 3 * per):
                    at = rel * per + row % per
                    params_out[row // per, at : at + 1, :] = stats_ref[
                        first + row // 8, row % 8 : row % 8 + 1, :
                    ]
            params = [params_out[3 * layer + i] for i in range(3)]
        else:
            params = [params_ref[3 * layer + i] for i in range(3)]
        _, mean, inv_std = norm_terms(stats_ref)
        to_relative(place_ref, spread, rows, mean, 0)
        to_relative(place_ref, spread, rows, inv_std, 1)
        rows[1] = rows[1] * params[0]
        rows[2] = params[1]
        rows[3] = params[2]
        held[...] = jnp.zeros_like(held)

    for row in range(blocks):
        drive_s[row * frames : (row + 1) * frames, :] = (
            columns_of(z_refs, row) - rows[0, row : row + 1, :]
        ) * rows[1, row : row + 1, :] + rows[2, row : row + 1, :]
    decay = rows[3]

    def step(t, state):
        at = pl.ds(t, blocks, stride=frames)
        pre = drive_s[at, :] + decay * state
        half = 0.5 + 0.5 * lax.erf(pre * (1.0 / ROOT_TWO))
        gate = gate_ref[chunk * frames + t] > 0.0
        slope = half + pre * jnp.exp(-0.5 * pre * pre) * (1.0 / ROOT_TWO_PI)
        state = jnp.where(gate, pre * half, state)
        state_s[at, :] = state
        slope_s[at, :] = jnp.where(gate, slope, 0.0)
        return state

    held[...] = lax.fori_loop(0, frames, step, held[...], unroll=8)
    valid = valid_ref[...]
    for row in range(blocks):
        lanes = slice(row * LANES, (row + 1) * LANES)
        state = state_s[row * frames : (row + 1) * frames, :]
        state_ref[:, lanes] = state
        slope_ref[:, lanes] = slope_s[row * frames : (row + 1) * frames, :]
        value = x_ref[:, lanes] + valid * state
        out, at = (outs[row // per], row % per) if last else (outs[0], row)
        out[:, at * LANES : (at + 1) * LANES] = value


def recur(layer, place, gate, z, stats, params, valid, x, last):
    frames, features = x.shape
    blocks = features // LANES
    some = frames // CHUNKS
    whole = lambda array: pl.BlockSpec(array.shape, lambda i: (0,) * array.ndim)
    by_chunk = lambda array: pl.BlockSpec((some, array.shape[1]), lambda i: (i, 0))
    full = jax.ShapeDtypeStruct((frames, features), F32)
    piece = jax.ShapeDtypeStruct((frames, features // 4), F32)
    out_shape = [piece] * 4 if last else [full]
    out_shape += [full, full]
    out_specs = [by_chunk(a) for a in out_shape]
    spread_params = params is None
    if spread_params:
        out_shape.append(jax.ShapeDtypeStruct((3 * LAYERS, blocks, LANES), F32))
        out_specs.append(whole(out_shape[-1]))
        params = valid
    return call(
        partial(recur_body, len(z), last, layer, spread_params),
        grid=(CHUNKS,),
        in_specs=[SMEM_SPEC, SMEM_SPEC]
        + [by_chunk(a) for a in z]
        + [whole(a) for a in (stats, params)]
        + [by_chunk(a) for a in (valid, x)],
        out_specs=out_specs,
        out_shape=out_shape,
        hbm_outs=tuple(range(len(out_shape) - spread_params)) if last else (1, 2),
        scratch_shapes=[
            pltpu.VMEM((4, blocks, LANES), F32),
            pltpu.VMEM((blocks, LANES), F32),
            pltpu.VMEM((blocks, LANES), F32),
        ]
        + [pltpu.VMEM((blocks * some, LANES), F32)] * 3,
        cost_estimate=cost(100 * frames * features, 20 * frames * features),
        name="recur",
    )(place, gate, *[in_hbm(a) for a in z], stats, params, valid, in_hbm(x))


def back_body(n_z, n_ups, spots, layer, place_ref, gate_ref, *refs):
    z_refs, refs = refs[:n_z], refs[n_z:]
    (stats_ref, params_ref), refs = refs[:2], refs[2:]
    ups, (state_ref, slope_ref), refs = refs[:n_ups], refs[n_ups : n_ups + 2], refs[n_ups + 2 :]
    grad_ref, sums_ref, rows, spread, held, up_s, state_s, slope_s = refs
    frames, features = state_ref.shape
    blocks = features // LANES
    per = blocks // 4
    tall = frames + 8
    step_no = pl.program_id(0)
    chunk = pl.num_programs(0) - 1 - step_no

    @pl.when(step_no == 0)
    def _():
        _, mean, inv_std = norm_terms(stats_ref)
        to_relative(place_ref, spread, rows, mean, 0)
        to_relative(place_ref, spread, rows, inv_std, 1)
        held[...] = jnp.zeros_like(held)

    for row in range(blocks):
        lanes = slice(row * LANES, (row + 1) * LANES)
        base = row * frames
        up = None
        for (_, column), part in zip(spots, ups):
            if column <= row * LANES < column + part.shape[1]:
                value = part[:, row * LANES - column : (row + 1) * LANES - column]
                up = value if up is None else up + value
        up_s[base : base + frames, :] = up
        state_s[row * tall : row * tall + 8, :] = jnp.zeros((8, LANES), F32)
        state_s[row * tall + 8 : (row + 1) * tall, :] = state_ref[:, lanes]
        slope_s[base : base + frames, :] = slope_ref[:, lanes]
    decay = params_ref[3 * layer + 2]

    def step(i, carry):
        t = frames - 1 - i
        at = pl.ds(t, blocks, stride=frames)
        slope = slope_s[at, :]
        gate = gate_ref[chunk * frames + t]
        total = gate * up_s[at, :] + carry
        up_s[at, :] = total * slope
        return total * (slope * decay + (1.0 - gate))

    held[0] = lax.fori_loop(0, frames, step, held[0], unroll=8)
    held[4] += held[1] * state_s[pl.ds(tall - 1, blocks, stride=tall), :]
    held[1] = up_s[pl.ds(0, blocks, stride=frames), :]
    for row in range(blocks):
        lanes = slice(row * LANES, (row + 1) * LANES)
        grad = up_s[row * frames : (row + 1) * frames, :]
        grad_ref[:, lanes] = grad
        zhat = (columns_of(z_refs, row) - rows[0, row : row + 1, :]) * rows[1, row : row + 1, :]
        before = state_s[row * tall + 7 : row * tall + 7 + frames, :]
        for slot, value in enumerate((grad * zhat, grad, grad * before)):
            held[2 + slot, row : row + 1, :] += jnp.sum(value, axis=0, keepdims=True)

    @pl.when(chunk == 0)
    def _():
        for row in range(blocks):
            at = place_ref[row // per] * per + row % per
            for slot in range(3):
                sums_ref[slot, pl.ds(at, 1), :] = held[2 + slot, row : row + 1, :]


def spots_of_sum(parts, width):
    spots, column = [], 0
    for array, _ in parts:
        spots.append((0, column % (4 * width)))
        column += array.shape[1]
    return spots


def back(layer, place, gate, z, stats, params, ups, states, slopes):
    frames, features = states.shape
    width = features // 4
    blocks = features // LANES
    some = frames // CHUNKS
    whole = lambda array: pl.BlockSpec(array.shape, lambda i: (0,) * array.ndim)

    def by_chunk(array, first=0):
        return pl.BlockSpec(
            (some, array.shape[1]), lambda i: ((first or 0) * CHUNKS + CHUNKS - 1 - i, 0)
        )

    out_shape = [
        jax.ShapeDtypeStruct((frames, features), F32),
        jax.ShapeDtypeStruct((3, blocks, LANES), F32),
    ]
    return call(
        partial(back_body, len(z), len(ups), spots_of_sum(ups, width), layer),
        grid=(CHUNKS,),
        in_specs=[SMEM_SPEC] * 2
        + [by_chunk(a) for a in z]
        + [whole(a) for a in (stats, params)]
        + [by_chunk(*up) for up in ups]
        + [by_chunk(a) for a in (states, slopes)],
        out_specs=[by_chunk(out_shape[0]), whole(out_shape[1])],
        out_shape=out_shape,
        scratch_shapes=[
            pltpu.VMEM((2, blocks, LANES), F32),
            pltpu.VMEM((blocks, LANES), F32),
            pltpu.VMEM((5, blocks, LANES), F32),
            pltpu.VMEM((blocks * some, LANES), F32),
            pltpu.VMEM((blocks * (some + 8), LANES), F32),
            pltpu.VMEM((blocks * some, LANES), F32),
        ],
        cost_estimate=cost(30 * frames * features, 20 * frames * features),
        name="back",
    )(
        place,
        gate,
        *[in_hbm(a) for a in z],
        stats,
        params,
        *arrays_of(ups),
        in_hbm(states),
        in_hbm(slopes),
    )


def input_terms(high_s, low_s, weights):
    left, right = [], []
    for block, weight in enumerate(weights):
        w_high, w_low = split(weight)
        left += [high_s[block], low_s[block], high_s[block]]
        right += [w_high, w_high, w_low]
    return dot(jnp.concatenate(left, axis=1), jnp.concatenate(right, axis=0), NN)


def norm_back_body(n_z, split_terms, layer, cols_ref, place_ref, grad_ref, *refs):
    del cols_ref
    z_refs, refs = refs[:n_z], refs[n_z:]
    params_ref, valid_ref, stats_ref, sums_ref, *refs = refs
    weights, refs = refs[:10], refs[10:]
    if split_terms:
        out_ref, leave_ref, near_term_ref, far_term_ref, sums_out_ref, *refs = refs
        term_refs, starts = (far_term_ref, near_term_ref), (0, 0)
    else:
        out_ref, leave_ref, term_ref, sums_out_ref, *refs = refs
        term_refs, starts = (term_ref, term_ref), (2 * grad_ref.shape[1] // 4, 0)
    rows, spread, high_s, low_s, far_ref = refs
    blocks = grad_ref.shape[1] // LANES
    width = high_s.shape[2]
    per = width // LANES

    @pl.when(pl.program_id(0) == 0)
    def _():
        count, mean, inv_std = norm_terms(stats_ref)
        to_relative(place_ref, spread, rows, mean, 0)
        to_relative(place_ref, spread, rows, inv_std, 1)
        rows[2] = rows[1] * params_ref[3 * layer]
        sums = [tree(gathered(sums_ref, slot)) for slot in range(3)]
        for slot in range(3):
            sums_out_ref[slot] = sums[slot]
        to_relative(place_ref, spread, rows, sums[0] / count, 3)
        to_relative(place_ref, spread, rows, sums[1] / count, 4)
        valid = valid_ref[...]
        for row in range(blocks):
            lanes = slice(row * LANES, (row + 1) * LANES)
            one = lambda slot: rows[slot, row : row + 1, :]
            zhat = (columns_of(z_refs, row) - one(0)) * one(1)
            value = one(2) * (grad_ref[:, lanes] - valid * (one(4) + zhat * one(3)))
            out_ref[:, lanes] = value
            if (row // per) % 2:
                at = (row // per // 2) * width + (row % per) * LANES
                leave_ref[:, at : at + LANES] = value
            high, low = split(value)
            inner = slice((row % per) * LANES, (row % per + 1) * LANES)
            high_s[row // per, :, inner] = high
            low_s[row // per, :, inner] = low

    value = input_terms(high_s, low_s, weight_blocks(place_ref, weights, far_ref))
    for step, (term_ref, first) in enumerate(zip(term_refs, starts)):

        @pl.when(pl.program_id(0) == step)
        def _():
            for pair in range(2):
                at = pl.multiple_of(((place_ref[0] & 1) ^ pair) * width, width)
                term_ref[:, pl.ds(first + at, width)] = value[
                    :, pair * width : (pair + 1) * width
                ]


def norm_back(columns, place, grad, z, params, valid, stats, sums, weights, layer, split_terms):
    frames, features = grad.shape
    width = features // 4
    blocks = features // LANES
    whole = lambda array: pl.BlockSpec(array.shape, lambda s, cols, place: (0,) * array.ndim)
    operands = [grad, *[in_hbm(a) for a in z], params, valid, stats, sums]
    full = jax.ShapeDtypeStruct((frames, features), F32)
    half = jax.ShapeDtypeStruct((frames, 2 * width), F32)
    terms = [half, half] if split_terms else [full]
    out_shape = [full, half, *terms, jax.ShapeDtypeStruct((3, blocks, LANES), F32)]
    return call(
        partial(norm_back_body, len(z), split_terms, layer),
        grid_spec=pltpu.PrefetchScalarGridSpec(
            num_scalar_prefetch=2,
            grid=(2,),
            in_specs=[whole(a) for a in operands] + weight_specs(weights, layer),
            out_specs=[whole(a) for a in out_shape],
            scratch_shapes=[
                pltpu.VMEM((5, blocks, LANES), F32),
                pltpu.VMEM((blocks, LANES), F32),
                pltpu.VMEM((4, frames, width), BF16),
                pltpu.VMEM((4, frames, width), BF16),
                far_scratch(width),
            ],
        ),
        out_shape=out_shape,
        hbm_outs=(0,),
        cost_estimate=cost(6 * frames * features * features, 4 * features * features),
        name="norm_back",
    )(columns, place, *operands, *[in_hbm(w) for w in weights])


def own_terms_body(n_ups, spots, cols_ref, place_ref, grad_ref, *refs):
    del cols_ref
    ups, refs = refs[:n_ups], refs[n_ups:]
    weights, refs = refs[:10], refs[10:]
    out_ref, high_s, low_s, far_ref = refs
    width = high_s.shape[2]
    step = pl.program_id(0)

    @pl.when(step == 0)
    def _():
        for block in range(4):
            high, low = split(grad_ref[:, block * width : (block + 1) * width])
            high_s[block] = high
            low_s[block] = low

    value = input_terms(high_s, low_s, weight_blocks(place_ref, weights, far_ref))
    for pair in range(2):
        at = pl.multiple_of(((place_ref[0] & 1) ^ pair) * width, width)
        out_ref[:, pl.ds(at, width)] = value[:, pair * width : (pair + 1) * width]
    for half in range(2):

        @pl.when(step == half)
        def _():
            first = 2 * half * width
            for (_, column), up in zip(spots, ups):
                low = max(column, first)
                high = min(column + up.shape[1], first + 2 * width)
                if low < high:
                    out_ref[:, low - first : high - first] += up[:, low - column : high - column]


def own_terms(columns, place, grad, ups, weights, layer):
    frames, features = grad.shape
    width = features // 4
    whole = lambda array: pl.BlockSpec(array.shape, lambda s, cols, place: (0,) * array.ndim)
    step_block = pl.BlockSpec((frames, 2 * width), lambda s, cols, place: (0, s))
    return call(
        partial(own_terms_body, len(ups), spots_of_sum(ups, width)),
        grid_spec=pltpu.PrefetchScalarGridSpec(
            num_scalar_prefetch=2,
            grid=(2,),
            in_specs=[whole(grad)]
            + [part_spec(up, frames) for up in ups]
            + weight_specs(weights, layer),
            out_specs=step_block,
            scratch_shapes=[pltpu.VMEM((4, frames, width), BF16)] * 2 + [far_scratch(width)],
        ),
        out_shape=jax.ShapeDtypeStruct((frames, features), F32),
        cost_estimate=cost(6 * frames * features * features, 4 * features * features),
        name="own_terms",
    )(columns, place, in_hbm(grad), *arrays_of(ups), *[in_hbm(w) for w in weights])


def prepare_body(n_chunks, lists_ref, place_ref, *refs):
    del lists_ref
    groups = []
    for _ in range(4):
        groups.append(refs[:n_chunks])
        refs = refs[n_chunks:]
    high_ref, low_ref = refs
    padded = high_ref.shape[0] // 2
    width = high_ref.shape[1] // 2
    for side in range(2):

        @pl.when(pl.program_id(0) // 2 == side)
        def _():
            for clip in range(2):
                for dc in range(2):
                    at = pl.multiple_of((place_ref[6] ^ clip ^ dc) * width, width)
                    row = clip * padded
                    for part in groups[2 * clip + side]:
                        rows = part.shape[0]
                        high, low = split(part[:, dc * width : (dc + 1) * width])
                        high_ref[row : row + rows, pl.ds(at, width)] = high
                        low_ref[row : row + rows, pl.ds(at, width)] = low
                        row += rows
                rest = (clip + 1) * padded - row
                zeros = jnp.zeros((rest, 2 * width), BF16)
                high_ref[row : row + rest, :] = zeros
                low_ref[row : row + rest, :] = zeros


def prepare(lists, place, groups):
    width = groups[0][0].shape[1] // 4
    frames = sum(part.shape[0] for part in groups[0])
    padded = -(-frames // LANES) * LANES
    in_specs = []
    for i, group in enumerate(groups):
        for part in group:
            if i % 2 == 0:
                index = lambda s, *_: (0, jnp.minimum(s, 1))
            else:
                index = lambda s, *_: (0, jnp.maximum(s - 2, 0))
            in_specs.append(pl.BlockSpec((part.shape[0], 2 * width), index))
    out = jax.ShapeDtypeStruct((2 * padded, 8 * width), BF16)
    out_spec = pl.BlockSpec((2 * padded, 2 * width), lambda s, cols, place: (0, cols[s]))
    return call(
        partial(prepare_body, len(groups[0])),
        grid_spec=pltpu.PrefetchScalarGridSpec(
            num_scalar_prefetch=2,
            grid=(4,),
            in_specs=in_specs,
            out_specs=[out_spec, out_spec],
        ),
        out_shape=[out, out],
        hbm_outs=(0, 1),
        cost_estimate=cost(0, 16 * frames * 8 * width),
        name="prepare",
    )(lists, place, *[in_hbm(part) for group in groups for part in group])


def product(g_high, g_low, x_high, x_low):
    return dot(g_high, x_high, NN) + (dot(g_high, x_low, NN) + dot(g_low, x_high, NN))


def weight_body(turn, place_ref, *refs):
    if turn:
        grad_ref, near_ref, x_high, x_low, kept, sent, g_high, g_low, t_high, t_low = refs

        @pl.when(pl.program_id(0) == 0)
        def _():
            frames, features = grad_ref.shape
            width = features // 4
            rows = width // 4
            padded = t_high.shape[1] // 2
            t_high[...] = jnp.zeros_like(t_high)
            t_low[...] = jnp.zeros_like(t_low)
            for clip in range(2):
                for dh in range(2):
                    if clip == 0:
                        part = grad_ref[:, 2 * dh * width : (2 * dh + 1) * width]
                    else:
                        part = near_ref[:, dh * width : (dh + 1) * width]
                    high, low = split(part.T)
                    at = (
                        slice(dh * width, (dh + 1) * width),
                        slice(clip * padded, clip * padded + frames),
                    )
                    t_high[at] = high
                    t_low[at] = low
            for group in range(8):
                first, second, dh = group // 4, group // 2 % 2, group % 2
                core = place_ref[6]
                y = place_ref[4] ^ (first * core + second * (1 - core))
                x = place_ref[5] ^ (first * (1 - core) + second * core)
                at = pl.multiple_of(dh * width + (2 * y + x) * rows, rows)
                g_high[group * rows : (group + 1) * rows, :] = t_high[pl.ds(at, rows), :]
                g_low[group * rows : (group + 1) * rows, :] = t_low[pl.ds(at, rows), :]

    else:
        g_high, g_low, x_high, x_low, kept, sent = refs
    half = g_high.shape[0] // 2
    value = product(g_high[...], g_low[...], x_high[...], x_low[...])
    kept[...] = value[:half].reshape(kept.shape)
    sent[...] = value[half:].reshape(sent.shape)


def weight_rows(half, place, grads, x_split, width):
    turn = half == 0
    whole = lambda array: pl.BlockSpec(array.shape, lambda s, place: (0,) * array.ndim)
    x_spec = pl.BlockSpec((x_split[0].shape[0], width), lambda s, place: (0, 4 * half + s))
    shape = (2, 2, width // 4, 4 * width)
    out_shape = [jax.ShapeDtypeStruct(shape, F32)] * 2
    out_specs = [pl.BlockSpec(shape[:3] + (width,), lambda s, place: (0, 0, 0, s))] * 2
    scratch = []
    if turn:
        turned = (2 * width, x_split[0].shape[0])
        out_shape += [jax.ShapeDtypeStruct(turned, BF16)] * 2
        out_specs += [whole(out_shape[-1])] * 2
        scratch = [pltpu.VMEM(turned, BF16)] * 2
    return call(
        partial(weight_body, turn),
        grid_spec=pltpu.PrefetchScalarGridSpec(
            num_scalar_prefetch=1,
            grid=(4,),
            in_specs=[whole(a) for a in grads] + [x_spec] * 2,
            out_specs=out_specs,
            scratch_shapes=scratch,
        ),
        out_shape=out_shape,
        hbm_outs=(0,),
        cost_estimate=cost(12 * x_split[0].shape[0] * width * 4 * width, 4 * 8 * width * width),
        name="weight_rows",
    )(place, *([in_hbm(grads[0]), grads[1]] if turn else grads), *[in_hbm(x) for x in x_split])


def step_body(n, widths, cut, *refs):
    ins, outs = refs[: 2 * n], refs[2 * n :]
    starts = [sum(widths[:i]) for i in range(len(widths))]
    column = 0
    for i in range(n):
        total = ins[2 * i][...] + ins[2 * i + 1][...]
        end = column + total.shape[-1]
        for j, (start, columns) in enumerate(zip(starts, widths)):
            low, high = max(start, column), min(start + columns, end)
            if low < high:
                to = (Ellipsis, slice(low - start, high - start))
                piece = total[..., low - column : high - column]
                if cut:
                    outs[2 * j][to] = piece[0]
                    outs[2 * j + 1][to] = piece[1]
                else:
                    outs[j][to] = piece
        column = end


def step_of(*pairs, cut=True, widths=None):
    shape = list(pairs[0][0].shape)
    widths = widths or [sum(pair[0].shape[-1] for pair in pairs)]
    outs = []
    for columns in widths:
        shape[-1] = columns
        out = jax.ShapeDtypeStruct(tuple(shape[1:] if cut else shape), F32)
        outs += [out] * (1 + cut)
    whole = lambda array: pl.BlockSpec(array.shape, lambda i: (0,) * array.ndim)
    operands = [array for pair in pairs for array in pair]
    return call(
        partial(step_body, len(pairs), widths, cut),
        grid=(1,),
        in_specs=[whole(a) for a in operands],
        out_specs=[whole(a) for a in outs],
        out_shape=outs,
        cost_estimate=cost(0, 4 * sum(a.size for a in operands)),
        name="reduction_step",
    )(*operands)


def plane_swap(array, step):
    pairs = []
    for i in range(8):
        over_x = (i % 2 == 0) == (step == 0)
        pairs.append((i, i ^ 2 if over_x else i ^ 4))
    return lax.ppermute(array, ("y", "x", "c"), pairs)


def plane_gather(share, *before):
    first = plane_swap(share, 0)
    second = plane_swap(share, 1)
    return [share, second, first, plane_swap(after(first, *before), 1)]


def assemble_body(groups, place_ref, *refs):
    out_ref = refs[-1]
    core = place_ref[6]
    column = 0
    for group in range(groups):
        rows, columns = refs[4 * group].shape
        for i in range(4):
            first, second = i // 2, i % 2
            y = place_ref[4] ^ (first * core + second * (1 - core))
            x = place_ref[5] ^ (first * (1 - core) + second * core)
            at = pl.multiple_of((2 * y + x) * rows, rows)
            out_ref[0, pl.ds(at, rows), column : column + columns] = refs[4 * group + i][...]
        column += columns


def assemble(place, groups, layer, onto=None):
    pieces = [piece for group in groups for piece in group]
    rows = 4 * pieces[0].shape[0]
    columns = sum(group[0].shape[1] for group in groups)
    aliases, extra, extra_specs = {}, [], []
    if onto is not None:
        aliases, extra = {1 + len(pieces): 0}, [onto]
        extra_specs = [pl.BlockSpec(memory_space=pl.ANY)]
    (out,) = call(
        partial(assemble_body, len(groups)),
        grid=(1,),
        out_shape=[jax.ShapeDtypeStruct((LAYERS, rows, columns), F32)],
        hbm_outs=(0,),
        in_specs=[SMEM_SPEC]
        + [pl.BlockSpec(p.shape, lambda i: (0, 0)) for p in pieces]
        + extra_specs,
        out_specs=[pl.BlockSpec((1, rows, columns), lambda i: (layer, 0, 0))],
        input_output_aliases=aliases,
        cost_estimate=cost(0, 8 * rows * columns),
        name="assemble",
    )(place, *[p if extra else in_hbm(p) for p in pieces], *extra)
    return out


def half_features(inputs, weights, gains, shifts, decays, biases, lengths, frame_mask, grad_out):
    width, slots = inputs.shape
    clips, frames = frame_mask.shape
    depth = weights.shape[2]
    blocks = 4 * width // LANES
    y, x, h, l, c = (lax.axis_index(name) for name in ("y", "x", "h", "l", "c"))
    b = 2 * y + x
    numbers = [2 * (h ^ (rel // 2)) + (c ^ (rel % 2)) for rel in range(4)] + [y, x, c]
    place = jnp.stack(numbers).astype(jnp.int32)
    own_blocks, other_blocks = (
        jnp.stack(
            [2 * (2 * (h ^ (rel // 2)) + half) + (c ^ (rel % 2)) for rel in range(4)]
        ).astype(jnp.int32)
        for half in (l, 1 - l)
    )
    own_columns = jnp.stack([2 * h + l, 2 * (1 - h) + l]).astype(jnp.int32)
    other_columns = jnp.stack([2 * (1 - h) + 1 - l, 2 * h + 1 - l]).astype(jnp.int32)
    all_columns = jnp.concatenate([own_columns, other_columns[::-1]])
    rows = width // 4

    clip = 2 * h + c
    seen = lax.dynamic_index_in_dim(frame_mask, clip, 0, keepdims=False)
    length = lax.dynamic_index_in_dim(lengths, clip, 0, keepdims=False)
    moments = jnp.arange(frames, dtype=jnp.int32)
    gate = ((moments < length) & ((seen == 1) | (moments == 0))).astype(F32)
    valid = jnp.broadcast_to(gate[:, None], (frames, LANES))

    def far_share(layer):
        return lax.dynamic_slice(weights, (layer, b * rows, 0), (1, rows, depth))[0]

    def over_h(array):
        return lax.ppermute(array, "h", FLIP2)

    def over_c(array):
        return lax.ppermute(array, "c", FLIP2)

    def over_second(array):
        return plane_swap(array, 1)

    def four_of(near_rows, far_rows):
        return [
            (near_rows, 0),
            (over_c(near_rows), 1),
            (far_rows, 0),
            (over_c(far_rows), 1),
        ]

    def far_pieces(share):
        both = lax.ppermute(share, ("y", "x"), DIAGONAL)
        return [share, lax.ppermute(share, "x", FLIP2), lax.ppermute(share, "y", FLIP2), both]

    near = over_c(weights)
    share = far_share(0)
    close, away = pack(place, after(inputs, share), frames)
    share = over_h(share)
    away = over_h(away)
    other_close = swap_half(close)
    up_close, up_away = pack(place, after(grad_out, close), frames, waits=True)
    share = after(share, up_close, valid, near, other_close)
    pieces = far_pieces(share)
    away = after(away, pieces[1:])
    half_weights = [[weights, near, *pieces, *map(over_c, after(pieces, away))]]
    own = four_of(after(close, away), away)
    others = four_of(other_close, swap_half(away))
    params = jnp.stack([gains, shifts + biases, decays], axis=1)
    own_params = params.reshape(LAYERS * 3 * width // LANES, LANES)
    params = None

    def gather(array, axes):
        return lax.all_gather(array, axes, tiled=True)

    weight = half_weights[0]
    early = jnp.concatenate([own_blocks, other_blocks[:2]])
    z, own_flat = project(place, frames, own + others[:2], early, weight, 0, flat=own)
    z, stats, other_flat = project(
        place,
        frames,
        others[2:],
        other_blocks[2:],
        weight,
        0,
        z,
        valid,
        params=own_params,
        flat=others,
    )
    z = [z]
    stats = gather(stats, ("h", "c"))
    share = over_c(lax.ppermute(after(far_share(1), stats), ("h", "c"), DIAGONAL))
    stats = gather(stats, ("y", "x"))
    x, states, slopes, params = recur(0, place, gate, z, stats, None, valid, own_flat, False)
    groups = [[own_flat], [other_flat]]
    groups += [[over_c(after(p, z[0])) for p in group] for group in groups]
    x_split = prepare(all_columns, place, after(groups, slopes))
    saved = [(groups, x_split, z, stats, states, slopes)]

    up_away = over_h(after(up_away, share))
    pieces = far_pieces(after(share, slopes, groups))
    near = [weights, near]
    other = swap_half(x)
    z, *_ = project(place, frames, [(after(x, x_split[0]), None)], own_blocks, near, 1)
    far = [*pieces, *map(over_c, after(pieces, z))]
    half_weights.append(near + far)
    z, stats = project(place, frames, [(other, None)], other_blocks, near, 1, z, valid)
    both = jnp.concatenate([own_blocks, other_blocks])
    z_far, stats = project(
        place,
        frames,
        [(x, None), (other, None)],
        both,
        far,
        1,
        None,
        valid,
        stats,
    )
    z = [z, z_far]
    upstream = four_of(up_close, after(up_away, z_far))
    stats = gather(gather(stats, ("y", "x")), ("h", "c"))
    *output, states, slopes = recur(1, place, gate, z, stats, params, valid, x, True)
    groups = [[x], [other]]
    groups += [[over_c(after(p, slopes)) for p in group] for group in groups]
    saved.append((groups, None, z, stats, states, slopes))
    diagonal = over_c(over_h(output[3]))

    ups = upstream
    results = [None] * LAYERS
    for layer in range(LAYERS - 1, -1, -1):
        groups, x_split, z, stats, states, slopes = saved[layer]
        weight = half_weights[layer]
        grad_pre, sums = back(layer, place, gate, z, stats, params, ups, states, slopes)
        sums = gather(sums, ("y", "x"))
        if layer == 0:
            later, go = step_of(*[(in_hbm(k), after(g, sums)) for k, g in zip(stay, come)])
            sums = after(sums, later)
            go = over_second(go)
        sums = gather(sums, ("h", "c"))
        if layer > 0:
            away = over_h(after(output[2], sums))
        grad_z, leaving, *terms, sums = norm_back(
            other_columns, place, grad_pre, z, params, valid, stats, sums, weight, layer,
            layer == 0,
        )
        leaving = over_c(leaving)
        if layer > 0:
            received = [swap_half(terms[0])]
            x_split = prepare(all_columns, place, after(groups, grad_z, diagonal))
        else:
            received = [None, swap_half(terms[1])]
            later, go = step_of((later, after(go, grad_z)))
            leaving = after(leaving, later)
            later = (later, over_h(go))
        *first, g_high, g_low = weight_rows(0, place, (grad_z, leaving), x_split, width)
        turned = (g_high, g_low)
        come = [plane_swap(first[1], 0)]
        if layer > 0:
            turned = after(turned, away)
            output = [(a, 0) for a in (output[0], over_c(output[1]), away, diagonal)]
        else:
            received[0] = swap_half(after(terms[0], received[1]))
        second = weight_rows(1, place, turned, x_split, width)
        come.append(plane_swap(second[1], 0))
        stay = (first[0], second[0])
        kept = own_terms(own_columns, place, after(grad_z, second[0]), ups, weight, layer)
        ups = [(kept, None)] + [(r, None) for r in received]
        results[layer] = lax.dynamic_index_in_dim(
            sums.reshape(3, 4, width), clip, axis=1, keepdims=False
        )

    away = merge(kept, 1, received[1])
    (later,) = step_of((later[0], after(later[1], away)), cut=False)
    away = over_h(away)
    later_first, later_second = plane_swap(later, 0), plane_swap(later, 1)
    total, go = step_of((in_hbm(stay[0]), after(come[0], later_first)), (in_hbm(stay[1]), come[1]))
    go = over_second(go)
    later = [later, later_second, later_first, plane_swap(after(later_first, total), 1)]
    far = [(away, 0), (over_c(away), 1)]
    total, go = step_of((total, after(go, far[1][0])))
    go = over_h(go)
    output = unpack(place, [(after(array, total), i) for array, i in output], frames, waited=True)
    grad_weights = assemble(place, after([later], output), 1)
    (share,) = step_of((total, after(go, grad_weights)), cut=False)
    gathered = plane_gather(share)
    close = merge(kept, 0, after(received[0], gathered[2]))
    grad_in = [(close, 0), (over_c(close[frames:]), 0)] + far
    grad_in = unpack(place, grad_in, frames)
    grad_weights = assemble(place, after([gathered], grad_in), 0, grad_weights)
    sums = jnp.stack(results)
    return (
        output,
        grad_in,
        grad_weights,
        sums[:, 0],
        sums[:, 1],
        sums[:, 2],
        sums[:, 1],
    )


def gelu_slope(value):
    return (
        0.5 * (1.0 + jax.scipy.special.erf(value / ROOT_TWO))
        + value * jnp.exp(-0.5 * value * value) / ROOT_TWO_PI
    )


def recur_step(decay, state, inputs):
    drive_t, valid_t = inputs
    pre = drive_t + decay * state
    state = state + valid_t * (jax.nn.gelu(pre, approximate=False) - state)
    return (state, state)


def back_step(decay, carry, inputs):
    upstream_t, valid_t, pre_t = inputs
    total = upstream_t + carry
    grad_pre = total * valid_t * gelu_slope(pre_t)
    carry = total * (1.0 - valid_t) + grad_pre * decay
    return (carry, grad_pre)


def add_piece(weight, piece):
    return jnp.dot(weight, piece, precision=HIGH, preferred_element_type=jnp.float32)


def weight_columns(grad_pre_norm, piece):
    return jnp.einsum("jf,kf->jk", grad_pre_norm, piece, precision=HIGH)


def split_features(inputs, weights, gains, shifts, decays, biases, lengths, frame_mask, grad_out):
    width, slots = inputs.shape
    clips, frames_len = frame_mask.shape
    frames = jnp.arange(frames_len, dtype=jnp.int32)
    valid_grid = (
        (frames[None, :] < lengths[:, None]) & ((frame_mask == 1) | (frames[None, :] == 0))
    ).astype(jnp.float32)
    valid = valid_grid.reshape(-1)
    valid_row = valid[None, :]
    valid_time = jnp.broadcast_to(valid_grid.T[:, :, None], (frames_len, clips, width)).reshape(
        frames_len, clips * width
    )
    count_local = jnp.sum(valid)

    def to_time(array):
        return jnp.transpose(array.reshape(width, clips, frames_len), (2, 1, 0)).reshape(
            frames_len, clips * width
        )

    def from_time(array):
        return jnp.transpose(array.reshape(frames_len, clips, width), (2, 1, 0)).reshape(
            width, slots
        )

    layer_in = inputs
    saved = []
    for layer_no in range(LAYERS):
        weight = weights[layer_no]
        gathered = lax.all_gather(layer_in, "neuron", axis=0, tiled=True)
        pre_norm = add_piece(weight, gathered)
        first_sum, count = lax.psum((jnp.sum(valid_row * pre_norm, axis=1), count_local), "batch")
        mean = first_sum / count
        centered = pre_norm - mean[:, None]
        var = lax.psum(jnp.sum(valid_row * centered * centered, axis=1), "batch") / count
        inv_std = lax.rsqrt(var + EPS)
        zhat = (pre_norm - mean[:, None]) * inv_std[:, None]
        drive = gains[layer_no][:, None] * zhat + (shifts[layer_no] + biases[layer_no])[:, None]
        drive_time = to_time(drive)
        decay_wide = jnp.tile(decays[layer_no], clips)
        start_state = jnp.zeros((clips * width,), jnp.float32)
        _, states = lax.scan(
            partial(recur_step, decay_wide), start_state, (drive_time, valid_time), unroll=8
        )
        saved.append((gathered, zhat, inv_std, drive_time, states, count))
        layer_in = layer_in + valid_row * from_time(states)
    upstream = grad_out
    grad_parts = [None] * LAYERS
    for layer_no in range(LAYERS - 1, -1, -1):
        gathered, zhat, inv_std, drive_time, states, count = saved[layer_no]
        decay_wide = jnp.tile(decays[layer_no], clips)
        gain = gains[layer_no]
        previous = jnp.concatenate([jnp.zeros_like(states[:1]), states[:-1]], axis=0)
        pre_time = drive_time + decay_wide[None, :] * previous
        grad_state = to_time(valid_row * upstream)
        start_carry = jnp.zeros((clips * width,), jnp.float32)
        _, grad_pre_time = lax.scan(
            partial(back_step, decay_wide),
            start_carry,
            (grad_state, valid_time, pre_time),
            reverse=True,
            unroll=8,
        )
        decay_local = jnp.sum(
            jnp.sum(grad_pre_time * previous, axis=0).reshape(clips, width), axis=0
        )
        grad_pre = from_time(grad_pre_time)
        gain_local = jnp.sum(grad_pre * zhat, axis=1)
        shift_local = jnp.sum(grad_pre, axis=1)
        grad_gain, grad_shift, grad_decay = lax.psum(
            (gain_local, shift_local, decay_local), "batch"
        )
        grad_pre_norm = (gain * inv_std)[:, None] * (
            grad_pre - valid_row * (grad_shift[:, None] + zhat * grad_gain[:, None]) / count
        )
        weight_local = weight_columns(grad_pre_norm, gathered)
        input_terms = jnp.einsum("jk,jf->kf", weights[layer_no], grad_pre_norm, precision=HIGH)
        input_grad = lax.psum_scatter(input_terms, "neuron", scatter_dimension=0, tiled=True)
        grad_weight = lax.psum(weight_local, "batch")
        upstream = upstream + input_grad
        grad_parts[layer_no] = (grad_weight, grad_gain, grad_shift, grad_decay)
    grad_weights = jnp.stack([grad_parts[layer_no][0] for layer_no in range(LAYERS)])
    grad_gains = jnp.stack([grad_parts[layer_no][1] for layer_no in range(LAYERS)])
    grad_shifts = jnp.stack([grad_parts[layer_no][2] for layer_no in range(LAYERS)])
    grad_decays = jnp.stack([grad_parts[layer_no][3] for layer_no in range(LAYERS)])
    return (layer_in, upstream, grad_weights, grad_gains, grad_shifts, grad_decays, grad_shifts)


def solution(mesh):
    if (mesh.shape["batch"], mesh.shape["neuron"]) == (4, 8):
        cut = Mesh(mesh.devices.reshape(2, 2, 2, 2, 2), ("y", "x", "h", "l", "c"))
        batch, neuron, body = ("y", "x"), ("h", "l", "c"), half_features
    else:
        cut, batch, neuron, body = mesh, "batch", "neuron", split_features
    in_specs = (
        P(neuron, batch),
        P(None, neuron, None),
        P(None, neuron),
        P(None, neuron),
        P(None, neuron),
        P(None, neuron),
        P(batch),
        P(batch, None),
        P(neuron, batch),
    )
    out_specs = (
        P(neuron, batch),
        P(neuron, batch),
        P(None, neuron, None),
        P(None, neuron),
        P(None, neuron),
        P(None, neuron),
        P(None, neuron),
    )
    return jax.shard_map(
        body, mesh=cut, in_specs=in_specs, out_specs=out_specs, check_vma=False
    )
```

```python
from functools import partial
import math

import jax
import jax.numpy as jnp
from jax import lax
from jax.experimental import pallas as pl
from jax.experimental.pallas import tpu as pltpu
from jax.sharding import Mesh, PartitionSpec as P

LAYERS = 2
EPS = 1e-05
HIGH = lax.Precision.HIGHEST
ROOT_TWO = math.sqrt(2.0)
ROOT_TWO_PI = math.sqrt(2.0 * math.pi)
F32 = jnp.float32
BF16 = jnp.bfloat16
LANES = 128
VMEM_LIMIT = 24 * 1024 * 1024
SMEM_SPEC = pl.BlockSpec(memory_space=pltpu.SMEM)
VMEM_SPEC = pl.BlockSpec(memory_space=pltpu.VMEM)


FLIP2 = [(0, 1), (1, 0)]
DIAGONAL = [(0, 3), (1, 2), (2, 1), (3, 0)]


def swap_half(array):
    return lax.ppermute(array, "l", FLIP2)


def after(value, *others):
    return lax.optimization_barrier((value, others))[0]


def split(value):
    high = value.astype(BF16)
    return high, (value - high.astype(F32)).astype(BF16)


def dot(a, b, dims):
    return lax.dot_general(a, b, (dims, ((), ())), preferred_element_type=F32)


NT = ((1,), (1,))
NN = ((1,), (0,))


def in_hbm(array):
    return pltpu.with_memory_space_constraint(array, pltpu.HBM)


def call(body, out_shape, hbm_outs=(), **kwargs):
    if hbm_outs:
        out_shape = [
            pltpu.HBM(a.shape, a.dtype) if i in hbm_outs else a for i, a in enumerate(out_shape)
        ]
    return pl.pallas_call(
        body,
        out_shape=out_shape,
        compiler_params=pltpu.CompilerParams(vmem_limit_bytes=VMEM_LIMIT),
        **kwargs,
    )


def cost(flops, byte_count):
    return pl.CostEstimate(flops=int(flops) // 64, bytes_accessed=int(byte_count) // 64, transcendentals=0)


def pack_body(frames, place_ref, in_ref, near_ref, far_ref, turned):
    slots = in_ref.shape[1]
    for start in range(0, slots, LANES):
        turned[start : start + LANES, :] = in_ref[:, start : start + LANES].T
    for rel in range(4):
        first = pl.multiple_of(place_ref[rel] * frames, 8)
        out = (near_ref, far_ref)[rel // 2]
        out[(rel % 2) * frames : (rel % 2 + 1) * frames, :] = turned[pl.ds(first, frames), :]


def pack(place, array, frames, waits=False):
    width, slots = array.shape
    out = jax.ShapeDtypeStruct((2 * frames, width), F32)
    return call(
        partial(pack_body, frames),
        grid=(1,),
        out_shape=[out, out],
        in_specs=[SMEM_SPEC, pl.BlockSpec((width, slots), lambda i: (0, 0))],
        out_specs=[pl.BlockSpec(out.shape, lambda i: (0, 0))] * 2,
        scratch_shapes=[pltpu.VMEM((slots, width), F32)],
        hbm_outs=(0, 1) if waits else (),
        cost_estimate=cost(0, 8 * width * slots),
        name="pack",
    )(place, in_hbm(array))


def part_spec(part, frames):
    array, i = part
    if i is None:
        return pl.BlockSpec(array.shape, lambda *_: (0,) * array.ndim)
    return pl.BlockSpec((frames, array.shape[1]), lambda *_: (i, 0))


def arrays_of(parts):
    return [array for array, _ in parts]


def unpack_body(frames, place_ref, *refs):
    ins, out_ref, turned = refs[:4], refs[4], refs[5]
    slots = out_ref.shape[1]
    for rel in range(4):
        first = pl.multiple_of(place_ref[rel] * frames, 8)
        turned[pl.ds(first, frames), :] = ins[rel][...]
    for start in range(0, slots, LANES):
        out_ref[:, start : start + LANES] = turned[start : start + LANES, :].T


def unpack(place, parts, frames, waited=False):
    width = parts[0][0].shape[1]
    slots = 4 * frames
    return call(
        partial(unpack_body, frames),
        grid=(1,),
        out_shape=jax.ShapeDtypeStruct((width, slots), F32),
        in_specs=[SMEM_SPEC] + [part_spec(part, frames) for part in parts],
        out_specs=pl.BlockSpec((width, slots), lambda i: (0, 0)),
        scratch_shapes=[pltpu.VMEM((slots, width), F32)],
        cost_estimate=cost(0, 8 * width * slots),
        name="unpack",
    )(place, *[in_hbm(a) if waited else a for a in arrays_of(parts)])


def merge_body(kept_ref, come_ref, out_ref):
    frames, columns = kept_ref.shape
    width = columns // 2
    for i in range(2):
        some = slice(i * width, (i + 1) * width)
        out_ref[i * frames : (i + 1) * frames, :] = kept_ref[:, some] + come_ref[:, some]


def merge(kept, half, come):
    frames, columns = come.shape
    return call(
        merge_body,
        grid=(1,),
        out_shape=jax.ShapeDtypeStruct((2 * frames, columns // 2), F32),
        in_specs=[
            pl.BlockSpec((frames, columns), lambda i: (0, half)),
            pl.BlockSpec((frames, columns), lambda i: (0, 0)),
        ],
        out_specs=pl.BlockSpec((2 * frames, columns // 2), lambda i: (0, 0)),
        cost_estimate=cost(0, 12 * frames * columns),
        name="merge",
    )(kept, come)


def project_body(n_parts, n_flat, spots, n_weights, first, with_acc, with_stats, with_params, cols_ref, place_ref, *refs):
    del cols_ref

    def take(n):
        nonlocal refs
        some, refs = refs[:n], refs[n:]
        return some

    parts, flat_parts, weights = take(n_parts), take(n_flat), take(n_weights)
    acc, valid, stats_in, params = take(with_acc), take(with_stats > 0), take(with_stats > 1), take(with_params)
    (out_ref,) = take(1)
    stats, flat = take(with_stats > 0), take(n_flat > 0)
    x_high, x_low, far_ref = refs
    step = pl.program_id(0)
    width = x_high.shape[2]

    @pl.when(step == 0)
    def _():
        for block, part in zip(spots, parts):
            for start in range(0, part.shape[1], width):
                high, low = split(part[:, start : start + width])
                x_high[block + start // width] = high
                x_low[block + start // width] = low
        column = 0
        for part in flat_parts:
            flat[0][:, column : column + part.shape[1]] = part[...]
            column += part.shape[1]
        if with_acc:
            out_ref[...] = acc[0][...]
        else:
            out_ref[...] = jnp.zeros_like(out_ref)

    stacked = jnp.concatenate([x_high[step], x_low[step], x_high[step]], axis=1)
    for block, weight in enumerate(weight_blocks(place_ref, weights, far_ref)):
        w_high, w_low = split(weight)
        columns = slice(block * width, (block + 1) * width)
        out_ref[:, columns] += dot(stacked, jnp.concatenate([w_high, w_high, w_low], axis=1), NT)

    if with_stats:
        (stats_ref,) = stats

        @pl.when(step == pl.num_programs(0) - 1)
        def _():
            if stats_in:
                stats_ref[...] = stats_in[0][...]
            own = jnp.sum(valid[0][...], axis=0, keepdims=True)
            per = width // LANES
            for row in range(out_ref.shape[1] // LANES):
                z = out_ref[:, row * LANES : (row + 1) * LANES]
                total = jnp.sum(valid[0][...] * z, axis=0, keepdims=True)
                centred = valid[0][...] * (z - total / own)
                squares = jnp.sum(centred * centred, axis=0, keepdims=True)
                at = place_ref[first + row // per] * per + row % per
                stats_ref[0, pl.ds(at, 1), :] = total
                stats_ref[1, pl.ds(at, 1), :] = squares
                stats_ref[2, pl.ds(at, 1), :] = own
            if with_params:
                rest = params[0].shape[0] - 8
                stats_ref[3] = params[0][:8, :]
                stats_ref[4] = jnp.zeros_like(stats_ref[4])
                stats_ref[4, :rest, :] = params[0][8:, :]


def weight_specs(weights, layer, pairs=2):
    specs = []
    for weight in weights:
        if weight.ndim == 3:
            shape = (1, weight.shape[1], pairs * weight.shape[1])
            specs.append(pl.BlockSpec(shape, lambda s, cols, *_: (layer, 0, cols[s])))
        else:
            shape = (weight.shape[0], pairs * 4 * weight.shape[0])
            specs.append(pl.BlockSpec(shape, lambda s, cols, *_: (0, cols[s])))
    return specs


def far_scratch(width, pairs=2):
    return pltpu.VMEM((2, width, pairs * width), F32)


def weight_blocks(place_ref, refs, far_ref):
    near = [ref[0] for ref in refs if len(ref.shape) == 3]
    pieces = [ref for ref in refs if len(ref.shape) == 2]
    far = []
    for i in range(len(pieces) // 4):
        for rel, piece in enumerate(pieces[4 * i : 4 * i + 4]):
            rows = piece.shape[0]
            row = 2 * (place_ref[4] ^ (rel // 2)) + (place_ref[5] ^ (rel % 2))
            far_ref[i, pl.ds(pl.multiple_of(row * rows, rows), rows), :] = piece[...]
        far.append(far_ref[i])
    return near + far


def project(
    place, frames, parts, blocks, weights, layer, acc=None, valid=None, stats=None, params=None, flat=()
):
    near = weights[0].ndim == 3
    units = sum(1 if w.ndim == 3 else 0.25 for w in weights)
    width = weights[0].shape[1] if near else 4 * weights[0].shape[0]
    n = blocks.shape[0]
    spots, block = [], 0
    for array, _ in parts:
        spots.append(block)
        block += array.shape[1] // width
    full = pl.BlockSpec(memory_space=pltpu.VMEM)
    in_specs = [part_spec(part, frames) for part in (*parts, *flat)]
    in_specs += weight_specs(weights, layer, 1)
    operands = arrays_of(parts) + arrays_of(flat) + [in_hbm(w) for w in weights]
    array = jax.ShapeDtypeStruct((frames, int(units) * width), F32)
    array_spec = pl.BlockSpec(array.shape, lambda s, cols, place: (0, 0))
    out_shape, out_specs = [array], [array_spec]
    if acc is not None:
        in_specs.append(array_spec)
        operands.append(in_hbm(acc))
    if valid is not None:
        in_specs.append(full)
        operands.append(valid)
        shape = (3 if params is None else 5, 4 * width // LANES, LANES)
        out_shape.append(jax.ShapeDtypeStruct(shape, F32))
        out_specs.append(pl.BlockSpec(shape, lambda s, cols, place: (0, 0, 0)))
    for extra in (stats, params):
        if extra is not None:
            in_specs.append(full)
            operands.append(extra)
    if flat:
        out_shape.append(jax.ShapeDtypeStruct((frames, 4 * width), F32))
        out_specs.append(pl.BlockSpec((frames, 4 * width), lambda s, cols, place: (0, 0)))
    return call(
        partial(
            project_body,
            len(parts),
            len(flat),
            spots,
            len(weights),
            0 if near else 2,
            acc is not None,
            (valid is not None) + (stats is not None),
            params is not None,
        ),
        grid_spec=pltpu.PrefetchScalarGridSpec(
            num_scalar_prefetch=2,
            grid=(n,),
            in_specs=in_specs,
            out_specs=out_specs,
            scratch_shapes=[pltpu.VMEM((n, frames, width), BF16)] * 2 + [far_scratch(width, 1)],
        ),
        out_shape=out_shape,
        hbm_outs=(0, len(out_shape) - 1) if flat else (0,),
        cost_estimate=cost(6 * frames * n * width * units * width, 4 * n * width * units * width),
        name="project",
    )(blocks, place, *operands)


def to_relative(place_ref, spread, rows_ref, value, slot):
    per = value.shape[0] // 4
    spread[...] = value
    for rel in range(4):
        first = place_ref[rel] * per
        for row in range(per):
            rows_ref[slot, rel * per + row : rel * per + row + 1, :] = spread[
                pl.ds(first + row, 1), :
            ]


def tree(values):
    while len(values) > 1:
        values = [a + b for a, b in zip(values[::2], values[1::2])]
    return values[0]


def gathered(ref, slot):
    return [ref[i] for i in range(slot, ref.shape[0], ref.shape[0] // 16)]


def norm_terms(stats_ref):
    each = [gathered(stats_ref, slot) for slot in range(3)]
    totals, squares, owns = each
    count = tree(owns)
    mean = tree(totals) / count
    away = [total / own - mean for total, own in zip(totals, owns)]
    spread = tree([s + n * a * a for s, n, a in zip(squares, owns, away)])
    return count, mean, lax.rsqrt(spread / count + EPS)


CHUNKS = 4


def columns_of(refs, row):
    for ref in refs:
        if row * LANES < ref.shape[1]:
            return ref[:, row * LANES : (row + 1) * LANES]
        row -= ref.shape[1] // LANES


def recur_body(n_z, last, layer, spread_params, place_ref, gate_ref, *refs):
    z_refs, refs = refs[:n_z], refs[n_z:]
    (stats_ref, params_ref, valid_ref, x_ref), refs = refs[:4], refs[4:]
    outs, refs = refs[: 1 + 3 * last], refs[1 + 3 * last :]
    if spread_params:
        state_ref, slope_ref, params_out, rows, spread, held, drive_s, state_s, slope_s = refs
    else:
        state_ref, slope_ref, rows, spread, held, drive_s, state_s, slope_s = refs
    frames, features = x_ref.shape
    blocks = features // LANES
    per = blocks // 4
    chunk = pl.program_id(0)

    @pl.when(chunk == 0)
    def _():
        if spread_params:
            for rel in range(4):
                first = place_ref[rel] * (stats_ref.shape[0] // 16) + 3
                for row in range(LAYERS * 3 * per):
                    at = rel * per + row % per
                    params_out[row // per, at : at + 1, :] = stats_ref[
                        first + row // 8, row % 8 : row % 8 + 1, :
                    ]
            params = [params_out[3 * layer + i] for i in range(3)]
        else:
            params = [params_ref[3 * layer + i] for i in range(3)]
        _, mean, inv_std = norm_terms(stats_ref)
        to_relative(place_ref, spread, rows, mean, 0)
        to_relative(place_ref, spread, rows, inv_std, 1)
        rows[1] = rows[1] * params[0]
        rows[2] = params[1]
        rows[3] = params[2]
        held[...] = jnp.zeros_like(held)

    for row in range(blocks):
        drive_s[row * frames : (row + 1) * frames, :] = (
            columns_of(z_refs, row) - rows[0, row : row + 1, :]
        ) * rows[1, row : row + 1, :] + rows[2, row : row + 1, :]
    decay = rows[3]

    def step(t, state):
        at = pl.ds(t, blocks, stride=frames)
        pre = drive_s[at, :] + decay * state
        half = 0.5 + 0.5 * lax.erf(pre * (1.0 / ROOT_TWO))
        gate = gate_ref[chunk * frames + t] > 0.0
        slope = half + pre * jnp.exp(-0.5 * pre * pre) * (1.0 / ROOT_TWO_PI)
        state = jnp.where(gate, pre * half, state)
        state_s[at, :] = state
        slope_s[at, :] = jnp.where(gate, slope, 0.0)
        return state

    held[...] = lax.fori_loop(0, frames, step, held[...], unroll=8)
    valid = valid_ref[...]
    for row in range(blocks):
        lanes = slice(row * LANES, (row + 1) * LANES)
        state = state_s[row * frames : (row + 1) * frames, :]
        state_ref[:, lanes] = state
        slope_ref[:, lanes] = slope_s[row * frames : (row + 1) * frames, :]
        value = x_ref[:, lanes] + valid * state
        out, at = (outs[row // per], row % per) if last else (outs[0], row)
        out[:, at * LANES : (at + 1) * LANES] = value


def recur(layer, place, gate, z, stats, params, valid, x, last):
    frames, features = x.shape
    blocks = features // LANES
    some = frames // CHUNKS
    whole = lambda array: pl.BlockSpec(array.shape, lambda i: (0,) * array.ndim)
    by_chunk = lambda array: pl.BlockSpec((some, array.shape[1]), lambda i: (i, 0))
    full = jax.ShapeDtypeStruct((frames, features), F32)
    piece = jax.ShapeDtypeStruct((frames, features // 4), F32)
    out_shape = [piece] * 4 if last else [full]
    out_shape += [full, full]
    out_specs = [by_chunk(a) for a in out_shape]
    spread_params = params is None
    if spread_params:
        out_shape.append(jax.ShapeDtypeStruct((3 * LAYERS, blocks, LANES), F32))
        out_specs.append(whole(out_shape[-1]))
        params = valid
    return call(
        partial(recur_body, len(z), last, layer, spread_params),
        grid=(CHUNKS,),
        in_specs=[SMEM_SPEC, SMEM_SPEC]
        + [by_chunk(a) for a in z]
        + [whole(a) for a in (stats, params)]
        + [by_chunk(a) for a in (valid, x)],
        out_specs=out_specs,
        out_shape=out_shape,
        hbm_outs=tuple(range(len(out_shape) - spread_params)) if last else (1, 2),
        scratch_shapes=[
            pltpu.VMEM((4, blocks, LANES), F32),
            pltpu.VMEM((blocks, LANES), F32),
            pltpu.VMEM((blocks, LANES), F32),
        ]
        + [pltpu.VMEM((blocks * some, LANES), F32)] * 3,
        cost_estimate=cost(100 * frames * features, 20 * frames * features),
        name="recur",
    )(place, gate, *[in_hbm(a) for a in z], stats, params, valid, in_hbm(x))


def back_body(n_z, n_ups, spots, layer, place_ref, gate_ref, *refs):
    z_refs, refs = refs[:n_z], refs[n_z:]
    (stats_ref, params_ref), refs = refs[:2], refs[2:]
    ups, (state_ref, slope_ref), refs = refs[:n_ups], refs[n_ups : n_ups + 2], refs[n_ups + 2 :]
    grad_ref, sums_ref, rows, spread, held, up_s, state_s, slope_s = refs
    frames, features = state_ref.shape
    blocks = features // LANES
    per = blocks // 4
    tall = frames + 8
    step_no = pl.program_id(0)
    chunk = pl.num_programs(0) - 1 - step_no

    @pl.when(step_no == 0)
    def _():
        _, mean, inv_std = norm_terms(stats_ref)
        to_relative(place_ref, spread, rows, mean, 0)
        to_relative(place_ref, spread, rows, inv_std, 1)
        held[...] = jnp.zeros_like(held)

    for row in range(blocks):
        lanes = slice(row * LANES, (row + 1) * LANES)
        base = row * frames
        up = None
        for (_, column), part in zip(spots, ups):
            if column <= row * LANES < column + part.shape[1]:
                value = part[:, row * LANES - column : (row + 1) * LANES - column]
                up = value if up is None else up + value
        up_s[base : base + frames, :] = up
        state_s[row * tall : row * tall + 8, :] = jnp.zeros((8, LANES), F32)
        state_s[row * tall + 8 : (row + 1) * tall, :] = state_ref[:, lanes]
        slope_s[base : base + frames, :] = slope_ref[:, lanes]
    decay = params_ref[3 * layer + 2]

    def step(i, carry):
        t = frames - 1 - i
        at = pl.ds(t, blocks, stride=frames)
        slope = slope_s[at, :]
        gate = gate_ref[chunk * frames + t]
        total = gate * up_s[at, :] + carry
        up_s[at, :] = total * slope
        return total * (slope * decay + (1.0 - gate))

    held[0] = lax.fori_loop(0, frames, step, held[0], unroll=8)
    held[4] += held[1] * state_s[pl.ds(tall - 1, blocks, stride=tall), :]
    held[1] = up_s[pl.ds(0, blocks, stride=frames), :]
    for row in range(blocks):
        lanes = slice(row * LANES, (row + 1) * LANES)
        grad = up_s[row * frames : (row + 1) * frames, :]
        grad_ref[:, lanes] = grad
        zhat = (columns_of(z_refs, row) - rows[0, row : row + 1, :]) * rows[1, row : row + 1, :]
        before = state_s[row * tall + 7 : row * tall + 7 + frames, :]
        for slot, value in enumerate((grad * zhat, grad, grad * before)):
            held[2 + slot, row : row + 1, :] += jnp.sum(value, axis=0, keepdims=True)

    @pl.when(chunk == 0)
    def _():
        for row in range(blocks):
            at = place_ref[row // per] * per + row % per
            for slot in range(3):
                sums_ref[slot, pl.ds(at, 1), :] = held[2 + slot, row : row + 1, :]


def spots_of_sum(parts, width):
    spots, column = [], 0
    for array, _ in parts:
        spots.append((0, column % (4 * width)))
        column += array.shape[1]
    return spots


def back(layer, place, gate, z, stats, params, ups, states, slopes):
    frames, features = states.shape
    width = features // 4
    blocks = features // LANES
    some = frames // CHUNKS
    whole = lambda array: pl.BlockSpec(array.shape, lambda i: (0,) * array.ndim)

    def by_chunk(array, first=0):
        return pl.BlockSpec(
            (some, array.shape[1]), lambda i: ((first or 0) * CHUNKS + CHUNKS - 1 - i, 0)
        )

    out_shape = [
        jax.ShapeDtypeStruct((frames, features), F32),
        jax.ShapeDtypeStruct((3, blocks, LANES), F32),
    ]
    return call(
        partial(back_body, len(z), len(ups), spots_of_sum(ups, width), layer),
        grid=(CHUNKS,),
        in_specs=[SMEM_SPEC] * 2
        + [by_chunk(a) for a in z]
        + [whole(a) for a in (stats, params)]
        + [by_chunk(*up) for up in ups]
        + [by_chunk(a) for a in (states, slopes)],
        out_specs=[by_chunk(out_shape[0]), whole(out_shape[1])],
        out_shape=out_shape,
        scratch_shapes=[
            pltpu.VMEM((2, blocks, LANES), F32),
            pltpu.VMEM((blocks, LANES), F32),
            pltpu.VMEM((5, blocks, LANES), F32),
            pltpu.VMEM((blocks * some, LANES), F32),
            pltpu.VMEM((blocks * (some + 8), LANES), F32),
            pltpu.VMEM((blocks * some, LANES), F32),
        ],
        cost_estimate=cost(30 * frames * features, 20 * frames * features),
        name="back",
    )(
        place,
        gate,
        *[in_hbm(a) for a in z],
        stats,
        params,
        *arrays_of(ups),
        in_hbm(states),
        in_hbm(slopes),
    )


def input_terms(high_s, low_s, weights):
    left, right = [], []
    for block, weight in enumerate(weights):
        w_high, w_low = split(weight)
        left += [high_s[block], low_s[block], high_s[block]]
        right += [w_high, w_high, w_low]
    return dot(jnp.concatenate(left, axis=1), jnp.concatenate(right, axis=0), NN)


def norm_back_body(n_z, split_terms, layer, cols_ref, place_ref, grad_ref, *refs):
    del cols_ref
    z_refs, refs = refs[:n_z], refs[n_z:]
    params_ref, valid_ref, stats_ref, sums_ref, *refs = refs
    weights, refs = refs[:10], refs[10:]
    if split_terms:
        out_ref, leave_ref, near_term_ref, far_term_ref, sums_out_ref, *refs = refs
        term_refs, starts = (far_term_ref, near_term_ref), (0, 0)
    else:
        out_ref, leave_ref, term_ref, sums_out_ref, *refs = refs
        term_refs, starts = (term_ref, term_ref), (2 * grad_ref.shape[1] // 4, 0)
    rows, spread, high_s, low_s, far_ref = refs
    blocks = grad_ref.shape[1] // LANES
    width = high_s.shape[2]
    per = width // LANES

    @pl.when(pl.program_id(0) == 0)
    def _():
        count, mean, inv_std = norm_terms(stats_ref)
        to_relative(place_ref, spread, rows, mean, 0)
        to_relative(place_ref, spread, rows, inv_std, 1)
        rows[2] = rows[1] * params_ref[3 * layer]
        sums = [tree(gathered(sums_ref, slot)) for slot in range(3)]
        for slot in range(3):
            sums_out_ref[slot] = sums[slot]
        to_relative(place_ref, spread, rows, sums[0] / count, 3)
        to_relative(place_ref, spread, rows, sums[1] / count, 4)
        valid = valid_ref[...]
        for row in range(blocks):
            lanes = slice(row * LANES, (row + 1) * LANES)
            one = lambda slot: rows[slot, row : row + 1, :]
            zhat = (columns_of(z_refs, row) - one(0)) * one(1)
            value = one(2) * (grad_ref[:, lanes] - valid * (one(4) + zhat * one(3)))
            out_ref[:, lanes] = value
            if (row // per) % 2:
                at = (row // per // 2) * width + (row % per) * LANES
                leave_ref[:, at : at + LANES] = value
            high, low = split(value)
            inner = slice((row % per) * LANES, (row % per + 1) * LANES)
            high_s[row // per, :, inner] = high
            low_s[row // per, :, inner] = low

    value = input_terms(high_s, low_s, weight_blocks(place_ref, weights, far_ref))
    for step, (term_ref, first) in enumerate(zip(term_refs, starts)):

        @pl.when(pl.program_id(0) == step)
        def _():
            for pair in range(2):
                at = pl.multiple_of(((place_ref[0] & 1) ^ pair) * width, width)
                term_ref[:, pl.ds(first + at, width)] = value[
                    :, pair * width : (pair + 1) * width
                ]


def norm_back(columns, place, grad, z, params, valid, stats, sums, weights, layer, split_terms):
    frames, features = grad.shape
    width = features // 4
    blocks = features // LANES
    whole = lambda array: pl.BlockSpec(array.shape, lambda s, cols, place: (0,) * array.ndim)
    operands = [grad, *[in_hbm(a) for a in z], params, valid, stats, sums]
    full = jax.ShapeDtypeStruct((frames, features), F32)
    half = jax.ShapeDtypeStruct((frames, 2 * width), F32)
    terms = [half, half] if split_terms else [full]
    out_shape = [full, half, *terms, jax.ShapeDtypeStruct((3, blocks, LANES), F32)]
    return call(
        partial(norm_back_body, len(z), split_terms, layer),
        grid_spec=pltpu.PrefetchScalarGridSpec(
            num_scalar_prefetch=2,
            grid=(2,),
            in_specs=[whole(a) for a in operands] + weight_specs(weights, layer),
            out_specs=[whole(a) for a in out_shape],
            scratch_shapes=[
                pltpu.VMEM((5, blocks, LANES), F32),
                pltpu.VMEM((blocks, LANES), F32),
                pltpu.VMEM((4, frames, width), BF16),
                pltpu.VMEM((4, frames, width), BF16),
                far_scratch(width),
            ],
        ),
        out_shape=out_shape,
        hbm_outs=(0,),
        cost_estimate=cost(6 * frames * features * features, 4 * features * features),
        name="norm_back",
    )(columns, place, *operands, *[in_hbm(w) for w in weights])


def own_terms_body(n_ups, spots, cols_ref, place_ref, grad_ref, *refs):
    del cols_ref
    ups, refs = refs[:n_ups], refs[n_ups:]
    weights, refs = refs[:10], refs[10:]
    out_ref, high_s, low_s, far_ref = refs
    width = high_s.shape[2]
    step = pl.program_id(0)

    @pl.when(step == 0)
    def _():
        for block in range(4):
            high, low = split(grad_ref[:, block * width : (block + 1) * width])
            high_s[block] = high
            low_s[block] = low

    value = input_terms(high_s, low_s, weight_blocks(place_ref, weights, far_ref))
    for pair in range(2):
        at = pl.multiple_of(((place_ref[0] & 1) ^ pair) * width, width)
        out_ref[:, pl.ds(at, width)] = value[:, pair * width : (pair + 1) * width]
    for half in range(2):

        @pl.when(step == half)
        def _():
            first = 2 * half * width
            for (_, column), up in zip(spots, ups):
                low = max(column, first)
                high = min(column + up.shape[1], first + 2 * width)
                if low < high:
                    out_ref[:, low - first : high - first] += up[:, low - column : high - column]


def own_terms(columns, place, grad, ups, weights, layer):
    frames, features = grad.shape
    width = features // 4
    whole = lambda array: pl.BlockSpec(array.shape, lambda s, cols, place: (0,) * array.ndim)
    step_block = pl.BlockSpec((frames, 2 * width), lambda s, cols, place: (0, s))
    return call(
        partial(own_terms_body, len(ups), spots_of_sum(ups, width)),
        grid_spec=pltpu.PrefetchScalarGridSpec(
            num_scalar_prefetch=2,
            grid=(2,),
            in_specs=[whole(grad)]
            + [part_spec(up, frames) for up in ups]
            + weight_specs(weights, layer),
            out_specs=step_block,
            scratch_shapes=[pltpu.VMEM((4, frames, width), BF16)] * 2 + [far_scratch(width)],
        ),
        out_shape=jax.ShapeDtypeStruct((frames, features), F32),
        cost_estimate=cost(6 * frames * features * features, 4 * features * features),
        name="own_terms",
    )(columns, place, in_hbm(grad), *arrays_of(ups), *[in_hbm(w) for w in weights])


def prepare_body(n_chunks, lists_ref, place_ref, *refs):
    del lists_ref
    groups = []
    for _ in range(4):
        groups.append(refs[:n_chunks])
        refs = refs[n_chunks:]
    high_ref, low_ref = refs
    padded = high_ref.shape[0] // 2
    width = high_ref.shape[1] // 2
    for side in range(2):

        @pl.when(pl.program_id(0) // 2 == side)
        def _():
            for clip in range(2):
                for dc in range(2):
                    at = pl.multiple_of((place_ref[6] ^ clip ^ dc) * width, width)
                    row = clip * padded
                    for part in groups[2 * clip + side]:
                        rows = part.shape[0]
                        high, low = split(part[:, dc * width : (dc + 1) * width])
                        high_ref[row : row + rows, pl.ds(at, width)] = high
                        low_ref[row : row + rows, pl.ds(at, width)] = low
                        row += rows
                rest = (clip + 1) * padded - row
                zeros = jnp.zeros((rest, 2 * width), BF16)
                high_ref[row : row + rest, :] = zeros
                low_ref[row : row + rest, :] = zeros


def prepare(lists, place, groups):
    width = groups[0][0].shape[1] // 4
    frames = sum(part.shape[0] for part in groups[0])
    padded = -(-frames // LANES) * LANES
    in_specs = []
    for i, group in enumerate(groups):
        for part in group:
            if i % 2 == 0:
                index = lambda s, *_: (0, jnp.minimum(s, 1))
            else:
                index = lambda s, *_: (0, jnp.maximum(s - 2, 0))
            in_specs.append(pl.BlockSpec((part.shape[0], 2 * width), index))
    out = jax.ShapeDtypeStruct((2 * padded, 8 * width), BF16)
    out_spec = pl.BlockSpec((2 * padded, 2 * width), lambda s, cols, place: (0, cols[s]))
    return call(
        partial(prepare_body, len(groups[0])),
        grid_spec=pltpu.PrefetchScalarGridSpec(
            num_scalar_prefetch=2,
            grid=(4,),
            in_specs=in_specs,
            out_specs=[out_spec, out_spec],
        ),
        out_shape=[out, out],
        hbm_outs=(0, 1),
        cost_estimate=cost(0, 16 * frames * 8 * width),
        name="prepare",
    )(lists, place, *[in_hbm(part) for group in groups for part in group])


def product(g_high, g_low, x_high, x_low):
    return dot(g_high, x_high, NN) + (dot(g_high, x_low, NN) + dot(g_low, x_high, NN))


def weight_body(turn, place_ref, *refs):
    if turn:
        grad_ref, near_ref, x_high, x_low, kept, sent, g_high, g_low, t_high, t_low = refs

        @pl.when(pl.program_id(0) == 0)
        def _():
            frames, features = grad_ref.shape
            width = features // 4
            rows = width // 4
            padded = t_high.shape[1] // 2
            t_high[...] = jnp.zeros_like(t_high)
            t_low[...] = jnp.zeros_like(t_low)
            for clip in range(2):
                for dh in range(2):
                    if clip == 0:
                        part = grad_ref[:, 2 * dh * width : (2 * dh + 1) * width]
                    else:
                        part = near_ref[:, dh * width : (dh + 1) * width]
                    high, low = split(part.T)
                    at = (
                        slice(dh * width, (dh + 1) * width),
                        slice(clip * padded, clip * padded + frames),
                    )
                    t_high[at] = high
                    t_low[at] = low
            for group in range(8):
                first, second, dh = group // 4, group // 2 % 2, group % 2
                core = place_ref[6]
                y = place_ref[4] ^ (first * core + second * (1 - core))
                x = place_ref[5] ^ (first * (1 - core) + second * core)
                at = pl.multiple_of(dh * width + (2 * y + x) * rows, rows)
                g_high[group * rows : (group + 1) * rows, :] = t_high[pl.ds(at, rows), :]
                g_low[group * rows : (group + 1) * rows, :] = t_low[pl.ds(at, rows), :]

    else:
        g_high, g_low, x_high, x_low, kept, sent = refs
    half = g_high.shape[0] // 2
    value = product(g_high[...], g_low[...], x_high[...], x_low[...])
    kept[...] = value[:half].reshape(kept.shape)
    sent[...] = value[half:].reshape(sent.shape)


def weight_rows(half, place, grads, x_split, width):
    turn = half == 0
    whole = lambda array: pl.BlockSpec(array.shape, lambda s, place: (0,) * array.ndim)
    x_spec = pl.BlockSpec((x_split[0].shape[0], width), lambda s, place: (0, 4 * half + s))
    shape = (2, 2, width // 4, 4 * width)
    out_shape = [jax.ShapeDtypeStruct(shape, F32)] * 2
    out_specs = [pl.BlockSpec(shape[:3] + (width,), lambda s, place: (0, 0, 0, s))] * 2
    scratch = []
    if turn:
        turned = (2 * width, x_split[0].shape[0])
        out_shape += [jax.ShapeDtypeStruct(turned, BF16)] * 2
        out_specs += [whole(out_shape[-1])] * 2
        scratch = [pltpu.VMEM(turned, BF16)] * 2
    return call(
        partial(weight_body, turn),
        grid_spec=pltpu.PrefetchScalarGridSpec(
            num_scalar_prefetch=1,
            grid=(4,),
            in_specs=[whole(a) for a in grads] + [x_spec] * 2,
            out_specs=out_specs,
            scratch_shapes=scratch,
        ),
        out_shape=out_shape,
        hbm_outs=(0,),
        cost_estimate=cost(12 * x_split[0].shape[0] * width * 4 * width, 4 * 8 * width * width),
        name="weight_rows",
    )(place, *([in_hbm(grads[0]), grads[1]] if turn else grads), *[in_hbm(x) for x in x_split])


def step_body(n, widths, cut, *refs):
    ins, outs = refs[: 2 * n], refs[2 * n :]
    starts = [sum(widths[:i]) for i in range(len(widths))]
    column = 0
    for i in range(n):
        total = ins[2 * i][...] + ins[2 * i + 1][...]
        end = column + total.shape[-1]
        for j, (start, columns) in enumerate(zip(starts, widths)):
            low, high = max(start, column), min(start + columns, end)
            if low < high:
                to = (Ellipsis, slice(low - start, high - start))
                piece = total[..., low - column : high - column]
                if cut:
                    outs[2 * j][to] = piece[0]
                    outs[2 * j + 1][to] = piece[1]
                else:
                    outs[j][to] = piece
        column = end


def step_of(*pairs, cut=True, widths=None):
    shape = list(pairs[0][0].shape)
    widths = widths or [sum(pair[0].shape[-1] for pair in pairs)]
    outs = []
    for columns in widths:
        shape[-1] = columns
        out = jax.ShapeDtypeStruct(tuple(shape[1:] if cut else shape), F32)
        outs += [out] * (1 + cut)
    whole = lambda array: pl.BlockSpec(array.shape, lambda i: (0,) * array.ndim)
    operands = [array for pair in pairs for array in pair]
    return call(
        partial(step_body, len(pairs), widths, cut),
        grid=(1,),
        in_specs=[whole(a) for a in operands],
        out_specs=[whole(a) for a in outs],
        out_shape=outs,
        cost_estimate=cost(0, 4 * sum(a.size for a in operands)),
        name="reduction_step",
    )(*operands)


def plane_swap(array, step):
    pairs = []
    for i in range(8):
        over_x = (i % 2 == 0) == (step == 0)
        pairs.append((i, i ^ 2 if over_x else i ^ 4))
    return lax.ppermute(array, ("y", "x", "c"), pairs)


def plane_gather(share, *before):
    first = plane_swap(share, 0)
    second = plane_swap(share, 1)
    return [share, second, first, plane_swap(after(first, *before), 1)]


def assemble_body(groups, place_ref, *refs):
    out_ref = refs[-1]
    core = place_ref[6]
    column = 0
    for group in range(groups):
        rows, columns = refs[4 * group].shape
        for i in range(4):
            first, second = i // 2, i % 2
            y = place_ref[4] ^ (first * core + second * (1 - core))
            x = place_ref[5] ^ (first * (1 - core) + second * core)
            at = pl.multiple_of((2 * y + x) * rows, rows)
            out_ref[0, pl.ds(at, rows), column : column + columns] = refs[4 * group + i][...]
        column += columns


def assemble(place, groups, layer, onto=None):
    pieces = [piece for group in groups for piece in group]
    rows = 4 * pieces[0].shape[0]
    columns = sum(group[0].shape[1] for group in groups)
    aliases, extra, extra_specs = {}, [], []
    if onto is not None:
        aliases, extra = {1 + len(pieces): 0}, [onto]
        extra_specs = [pl.BlockSpec(memory_space=pl.ANY)]
    (out,) = call(
        partial(assemble_body, len(groups)),
        grid=(1,),
        out_shape=[jax.ShapeDtypeStruct((LAYERS, rows, columns), F32)],
        hbm_outs=(0,),
        in_specs=[SMEM_SPEC]
        + [pl.BlockSpec(p.shape, lambda i: (0, 0)) for p in pieces]
        + extra_specs,
        out_specs=[pl.BlockSpec((1, rows, columns), lambda i: (layer, 0, 0))],
        input_output_aliases=aliases,
        cost_estimate=cost(0, 8 * rows * columns),
        name="assemble",
    )(place, *[p if extra else in_hbm(p) for p in pieces], *extra)
    return out


def half_features(inputs, weights, gains, shifts, decays, biases, lengths, frame_mask, grad_out):
    width, slots = inputs.shape
    clips, frames = frame_mask.shape
    depth = weights.shape[2]
    blocks = 4 * width // LANES
    y, x, h, l, c = (lax.axis_index(name) for name in ("y", "x", "h", "l", "c"))
    b = 2 * y + x
    numbers = [2 * (h ^ (rel // 2)) + (c ^ (rel % 2)) for rel in range(4)] + [y, x, c]
    place = jnp.stack(numbers).astype(jnp.int32)
    own_blocks, other_blocks = (
        jnp.stack(
            [2 * (2 * (h ^ (rel // 2)) + half) + (c ^ (rel % 2)) for rel in range(4)]
        ).astype(jnp.int32)
        for half in (l, 1 - l)
    )
    own_columns = jnp.stack([2 * h + l, 2 * (1 - h) + l]).astype(jnp.int32)
    other_columns = jnp.stack([2 * (1 - h) + 1 - l, 2 * h + 1 - l]).astype(jnp.int32)
    all_columns = jnp.concatenate([own_columns, other_columns[::-1]])
    rows = width // 4

    clip = 2 * h + c
    seen = lax.dynamic_index_in_dim(frame_mask, clip, 0, keepdims=False)
    length = lax.dynamic_index_in_dim(lengths, clip, 0, keepdims=False)
    moments = jnp.arange(frames, dtype=jnp.int32)
    gate = ((moments < length) & ((seen == 1) | (moments == 0))).astype(F32)
    valid = jnp.broadcast_to(gate[:, None], (frames, LANES))

    def far_share(layer):
        return lax.dynamic_slice(weights, (layer, b * rows, 0), (1, rows, depth))[0]

    def over_h(array):
        return lax.ppermute(array, "h", FLIP2)

    def over_c(array):
        return lax.ppermute(array, "c", FLIP2)

    def over_second(array):
        return plane_swap(array, 1)

    def four_of(near_rows, far_rows):
        return [
            (near_rows, 0),
            (over_c(near_rows), 1),
            (far_rows, 0),
            (over_c(far_rows), 1),
        ]

    def far_pieces(share):
        both = lax.ppermute(share, ("y", "x"), DIAGONAL)
        return [share, lax.ppermute(share, "x", FLIP2), lax.ppermute(share, "y", FLIP2), both]

    near = over_c(weights)
    share = far_share(0)
    close, away = pack(place, after(inputs, share), frames)
    share = over_h(share)
    away = over_h(away)
    other_close = swap_half(close)
    up_close, up_away = pack(place, after(grad_out, close), frames, waits=True)
    share = after(share, up_close, valid, near, other_close)
    pieces = far_pieces(share)
    away = after(away, pieces[1:])
    half_weights = [[weights, near, *pieces, *map(over_c, after(pieces, away))]]
    own = four_of(after(close, away), away)
    other_away = swap_half(away)
    others = [(other_close, 0), (over_c(other_close), 1)]
    params = jnp.stack([gains, shifts + biases, decays], axis=1)
    own_params = params.reshape(LAYERS * 3 * width // LANES, LANES)
    params = None

    def gather(array, axes):
        return lax.all_gather(array, axes, tiled=True)

    weight = half_weights[0]
    early = jnp.concatenate([own_blocks, other_blocks[:2]])
    z, own_flat = project(place, frames, own + others, early, weight, 0, flat=own)
    others += [(other_away, 0), (over_c(after(other_away, z)), 1)]
    z, stats, other_flat = project(
        place,
        frames,
        others[2:],
        other_blocks[2:],
        weight,
        0,
        z,
        valid,
        params=own_params,
        flat=others,
    )
    z = [z]
    stats = gather(stats, ("h", "c"))
    share = over_c(lax.ppermute(after(far_share(1), stats), ("h", "c"), DIAGONAL))
    stats = gather(stats, ("y", "x"))
    x, states, slopes, params = recur(0, place, gate, z, stats, None, valid, own_flat, False)
    groups = [[own_flat], [other_flat]]
    groups += [[over_c(after(p, z[0])) for p in group] for group in groups]
    x_split = prepare(all_columns, place, after(groups, slopes))
    saved = [(groups, x_split, z, stats, states, slopes)]

    pieces = far_pieces(after(share, slopes, groups))
    near = [weights, near]
    other = swap_half(x)
    z, *_ = project(place, frames, [(after(x, x_split[0]), None)], own_blocks, near, 1)
    far = [*pieces, *map(over_c, after(pieces, z))]
    up_away = over_h(after(up_away, other, z))
    half_weights.append(near + far)
    z, stats = project(place, frames, [(other, None)], other_blocks, near, 1, z, valid)
    both = jnp.concatenate([own_blocks, other_blocks])
    z_far, stats = project(
        place,
        frames,
        [(x, None), (other, None)],
        both,
        far,
        1,
        None,
        valid,
        stats,
    )
    z = [z, z_far]
    upstream = four_of(up_close, after(up_away, z_far))
    stats = gather(gather(stats, ("y", "x")), ("h", "c"))
    *output, states, slopes = recur(1, place, gate, z, stats, params, valid, x, True)
    groups = [[x], [other]]
    groups += [[over_c(after(p, slopes)) for p in group] for group in groups]
    saved.append((groups, None, z, stats, states, slopes))
    diagonal = over_c(over_h(output[3]))

    ups = upstream
    results = [None] * LAYERS
    for layer in range(LAYERS - 1, -1, -1):
        groups, x_split, z, stats, states, slopes = saved[layer]
        weight = half_weights[layer]
        grad_pre, sums = back(layer, place, gate, z, stats, params, ups, states, slopes)
        sums = gather(sums, ("y", "x"))
        if layer == 0:
            later, go = step_of(*[(in_hbm(k), after(g, sums)) for k, g in zip(stay, come)])
            sums = after(sums, later)
            go = over_second(go)
        sums = gather(sums, ("h", "c"))
        if layer > 0:
            away = over_h(after(output[2], sums))
        grad_z, leaving, *terms, sums = norm_back(
            other_columns, place, grad_pre, z, params, valid, stats, sums, weight, layer,
            layer == 0,
        )
        leaving = over_c(leaving)
        if layer > 0:
            received = [swap_half(terms[0])]
            x_split = prepare(all_columns, place, after(groups, grad_z, diagonal))
        else:
            received = [None, swap_half(terms[1])]
            later, go = step_of((later, after(go, grad_z)))
            leaving = after(leaving, later)
            later = (later, over_h(go))
        *first, g_high, g_low = weight_rows(0, place, (grad_z, leaving), x_split, width)
        turned = (g_high, g_low)
        come = [plane_swap(first[1], 0)]
        if layer > 0:
            turned = after(turned, away)
            output = [(a, 0) for a in (output[0], over_c(output[1]), away, diagonal)]
        else:
            received[0] = swap_half(after(terms[0], received[1]))
        second = weight_rows(1, place, turned, x_split, width)
        come.append(plane_swap(second[1], 0))
        stay = (first[0], second[0])
        kept = own_terms(own_columns, place, after(grad_z, second[0]), ups, weight, layer)
        ups = [(kept, None)] + [(r, None) for r in received]
        results[layer] = lax.dynamic_index_in_dim(
            sums.reshape(3, 4, width), clip, axis=1, keepdims=False
        )

    sums = jnp.stack(results)
    sums = [sums[:, 0], sums[:, 1], sums[:, 2]]
    away = merge(kept, 1, received[1])
    (later,) = step_of((later[0], after(later[1], away)), cut=False)
    away = over_h(away)
    later_first, later_second = plane_swap(later, 0), plane_swap(later, 1)
    come[0] = after(come[0], later_first, sums)
    total, go = step_of((in_hbm(stay[0]), come[0]), (in_hbm(stay[1]), come[1]))
    go = over_second(go)
    later = [later, later_second, later_first, plane_swap(after(later_first, total), 1)]
    far = [(away, 0), (over_c(away), 1)]
    total, go = step_of((total, after(go, far[1][0])))
    go = over_h(go)
    output = unpack(place, [(after(array, total), i) for array, i in output], frames, waited=True)
    grad_weights = assemble(place, after([later], output), 1)
    close = merge(kept, 0, after(received[0], grad_weights))
    (share,) = step_of((total, after(go, close)), cut=False)
    gathered = plane_gather(share)
    grad_in = [(close, 0), (over_c(close[frames:]), 0)] + far
    grad_in = unpack(place, grad_in, frames)
    grad_weights = assemble(place, after([gathered], grad_in), 0, grad_weights)
    return (output, grad_in, grad_weights, *sums, sums[1])


def gelu_slope(value):
    return (
        0.5 * (1.0 + jax.scipy.special.erf(value / ROOT_TWO))
        + value * jnp.exp(-0.5 * value * value) / ROOT_TWO_PI
    )


def recur_step(decay, state, inputs):
    drive_t, valid_t = inputs
    pre = drive_t + decay * state
    state = state + valid_t * (jax.nn.gelu(pre, approximate=False) - state)
    return (state, state)


def back_step(decay, carry, inputs):
    upstream_t, valid_t, pre_t = inputs
    total = upstream_t + carry
    grad_pre = total * valid_t * gelu_slope(pre_t)
    carry = total * (1.0 - valid_t) + grad_pre * decay
    return (carry, grad_pre)


def add_piece(weight, piece):
    return jnp.dot(weight, piece, precision=HIGH, preferred_element_type=jnp.float32)


def weight_columns(grad_pre_norm, piece):
    return jnp.einsum("jf,kf->jk", grad_pre_norm, piece, precision=HIGH)


def split_features(inputs, weights, gains, shifts, decays, biases, lengths, frame_mask, grad_out):
    width, slots = inputs.shape
    clips, frames_len = frame_mask.shape
    frames = jnp.arange(frames_len, dtype=jnp.int32)
    valid_grid = (
        (frames[None, :] < lengths[:, None]) & ((frame_mask == 1) | (frames[None, :] == 0))
    ).astype(jnp.float32)
    valid = valid_grid.reshape(-1)
    valid_row = valid[None, :]
    valid_time = jnp.broadcast_to(valid_grid.T[:, :, None], (frames_len, clips, width)).reshape(
        frames_len, clips * width
    )
    count_local = jnp.sum(valid)

    def to_time(array):
        return jnp.transpose(array.reshape(width, clips, frames_len), (2, 1, 0)).reshape(
            frames_len, clips * width
        )

    def from_time(array):
        return jnp.transpose(array.reshape(frames_len, clips, width), (2, 1, 0)).reshape(
            width, slots
        )

    layer_in = inputs
    saved = []
    for layer_no in range(LAYERS):
        weight = weights[layer_no]
        gathered = lax.all_gather(layer_in, "neuron", axis=0, tiled=True)
        pre_norm = add_piece(weight, gathered)
        first_sum, count = lax.psum((jnp.sum(valid_row * pre_norm, axis=1), count_local), "batch")
        mean = first_sum / count
        centered = pre_norm - mean[:, None]
        var = lax.psum(jnp.sum(valid_row * centered * centered, axis=1), "batch") / count
        inv_std = lax.rsqrt(var + EPS)
        zhat = (pre_norm - mean[:, None]) * inv_std[:, None]
        drive = gains[layer_no][:, None] * zhat + (shifts[layer_no] + biases[layer_no])[:, None]
        drive_time = to_time(drive)
        decay_wide = jnp.tile(decays[layer_no], clips)
        start_state = jnp.zeros((clips * width,), jnp.float32)
        _, states = lax.scan(
            partial(recur_step, decay_wide), start_state, (drive_time, valid_time), unroll=8
        )
        saved.append((gathered, zhat, inv_std, drive_time, states, count))
        layer_in = layer_in + valid_row * from_time(states)
    upstream = grad_out
    grad_parts = [None] * LAYERS
    for layer_no in range(LAYERS - 1, -1, -1):
        gathered, zhat, inv_std, drive_time, states, count = saved[layer_no]
        decay_wide = jnp.tile(decays[layer_no], clips)
        gain = gains[layer_no]
        previous = jnp.concatenate([jnp.zeros_like(states[:1]), states[:-1]], axis=0)
        pre_time = drive_time + decay_wide[None, :] * previous
        grad_state = to_time(valid_row * upstream)
        start_carry = jnp.zeros((clips * width,), jnp.float32)
        _, grad_pre_time = lax.scan(
            partial(back_step, decay_wide),
            start_carry,
            (grad_state, valid_time, pre_time),
            reverse=True,
            unroll=8,
        )
        decay_local = jnp.sum(
            jnp.sum(grad_pre_time * previous, axis=0).reshape(clips, width), axis=0
        )
        grad_pre = from_time(grad_pre_time)
        gain_local = jnp.sum(grad_pre * zhat, axis=1)
        shift_local = jnp.sum(grad_pre, axis=1)
        grad_gain, grad_shift, grad_decay = lax.psum(
            (gain_local, shift_local, decay_local), "batch"
        )
        grad_pre_norm = (gain * inv_std)[:, None] * (
            grad_pre - valid_row * (grad_shift[:, None] + zhat * grad_gain[:, None]) / count
        )
        weight_local = weight_columns(grad_pre_norm, gathered)
        input_terms = jnp.einsum("jk,jf->kf", weights[layer_no], grad_pre_norm, precision=HIGH)
        input_grad = lax.psum_scatter(input_terms, "neuron", scatter_dimension=0, tiled=True)
        grad_weight = lax.psum(weight_local, "batch")
        upstream = upstream + input_grad
        grad_parts[layer_no] = (grad_weight, grad_gain, grad_shift, grad_decay)
    grad_weights = jnp.stack([grad_parts[layer_no][0] for layer_no in range(LAYERS)])
    grad_gains = jnp.stack([grad_parts[layer_no][1] for layer_no in range(LAYERS)])
    grad_shifts = jnp.stack([grad_parts[layer_no][2] for layer_no in range(LAYERS)])
    grad_decays = jnp.stack([grad_parts[layer_no][3] for layer_no in range(LAYERS)])
    return (layer_in, upstream, grad_weights, grad_gains, grad_shifts, grad_decays, grad_shifts)


def solution(mesh):
    if (mesh.shape["batch"], mesh.shape["neuron"]) == (4, 8):
        cut = Mesh(mesh.devices.reshape(2, 2, 2, 2, 2), ("y", "x", "h", "l", "c"))
        batch, neuron, body = ("y", "x"), ("h", "l", "c"), half_features
    else:
        cut, batch, neuron, body = mesh, "batch", "neuron", split_features
    in_specs = (
        P(neuron, batch),
        P(None, neuron, None),
        P(None, neuron),
        P(None, neuron),
        P(None, neuron),
        P(None, neuron),
        P(batch),
        P(batch, None),
        P(neuron, batch),
    )
    out_specs = (
        P(neuron, batch),
        P(neuron, batch),
        P(None, neuron, None),
        P(None, neuron),
        P(None, neuron),
        P(None, neuron),
        P(None, neuron),
    )
    return jax.shard_map(
        body, mesh=cut, in_specs=in_specs, out_specs=out_specs, check_vma=False
    )
```

```python
from functools import partial
import math

import jax
import jax.numpy as jnp
from jax import lax
from jax.experimental import pallas as pl
from jax.experimental.pallas import tpu as pltpu
from jax.sharding import Mesh, PartitionSpec as P

LAYERS = 2
EPS = 1e-05
HIGH = lax.Precision.HIGHEST
ROOT_TWO = math.sqrt(2.0)
ROOT_TWO_PI = math.sqrt(2.0 * math.pi)
F32 = jnp.float32
BF16 = jnp.bfloat16
LANES = 128
VMEM_LIMIT = 24 * 1024 * 1024
SMEM_SPEC = pl.BlockSpec(memory_space=pltpu.SMEM)
VMEM_SPEC = pl.BlockSpec(memory_space=pltpu.VMEM)


FLIP2 = [(0, 1), (1, 0)]
DIAGONAL = [(0, 3), (1, 2), (2, 1), (3, 0)]


def swap_half(array):
    return lax.ppermute(array, "l", FLIP2)


def after(value, *others):
    return lax.optimization_barrier((value, others))[0]


def split(value):
    high = value.astype(BF16)
    return high, (value - high.astype(F32)).astype(BF16)


def dot(a, b, dims):
    return lax.dot_general(a, b, (dims, ((), ())), preferred_element_type=F32)


NT = ((1,), (1,))
NN = ((1,), (0,))


def in_hbm(array):
    return pltpu.with_memory_space_constraint(array, pltpu.HBM)


def call(body, out_shape, hbm_outs=(), **kwargs):
    if hbm_outs:
        out_shape = [
            pltpu.HBM(a.shape, a.dtype) if i in hbm_outs else a for i, a in enumerate(out_shape)
        ]
    return pl.pallas_call(
        body,
        out_shape=out_shape,
        compiler_params=pltpu.CompilerParams(vmem_limit_bytes=VMEM_LIMIT),
        **kwargs,
    )


def cost(flops, byte_count):
    return pl.CostEstimate(flops=int(flops) // 64, bytes_accessed=int(byte_count) // 64, transcendentals=0)


def pack_body(frames, place_ref, in_ref, near_ref, far_ref, turned):
    slots = in_ref.shape[1]
    for start in range(0, slots, LANES):
        turned[start : start + LANES, :] = in_ref[:, start : start + LANES].T
    for rel in range(4):
        first = pl.multiple_of(place_ref[rel] * frames, 8)
        out = (near_ref, far_ref)[rel // 2]
        out[(rel % 2) * frames : (rel % 2 + 1) * frames, :] = turned[pl.ds(first, frames), :]


def pack(place, array, frames, waits=False):
    width, slots = array.shape
    out = jax.ShapeDtypeStruct((2 * frames, width), F32)
    return call(
        partial(pack_body, frames),
        grid=(1,),
        out_shape=[out, out],
        in_specs=[SMEM_SPEC, pl.BlockSpec((width, slots), lambda i: (0, 0))],
        out_specs=[pl.BlockSpec(out.shape, lambda i: (0, 0))] * 2,
        scratch_shapes=[pltpu.VMEM((slots, width), F32)],
        hbm_outs=(0, 1) if waits else (),
        cost_estimate=cost(0, 8 * width * slots),
        name="pack",
    )(place, in_hbm(array))


def part_spec(part, frames):
    array, i = part
    if i is None:
        return pl.BlockSpec(array.shape, lambda *_: (0,) * array.ndim)
    return pl.BlockSpec((frames, array.shape[1]), lambda *_: (i, 0))


def arrays_of(parts):
    return [array for array, _ in parts]


def unpack_body(frames, place_ref, *refs):
    ins, out_ref, turned = refs[:4], refs[4], refs[5]
    slots = out_ref.shape[1]
    for rel in range(4):
        first = pl.multiple_of(place_ref[rel] * frames, 8)
        turned[pl.ds(first, frames), :] = ins[rel][...]
    for start in range(0, slots, LANES):
        out_ref[:, start : start + LANES] = turned[start : start + LANES, :].T


def unpack(place, parts, frames, waited=False):
    width = parts[0][0].shape[1]
    slots = 4 * frames
    return call(
        partial(unpack_body, frames),
        grid=(1,),
        out_shape=jax.ShapeDtypeStruct((width, slots), F32),
        in_specs=[SMEM_SPEC] + [part_spec(part, frames) for part in parts],
        out_specs=pl.BlockSpec((width, slots), lambda i: (0, 0)),
        scratch_shapes=[pltpu.VMEM((slots, width), F32)],
        cost_estimate=cost(0, 8 * width * slots),
        name="unpack",
    )(place, *[in_hbm(a) if waited else a for a in arrays_of(parts)])


def merge_body(kept_ref, come_ref, out_ref):
    frames, columns = kept_ref.shape
    width = columns // 2
    for i in range(2):
        some = slice(i * width, (i + 1) * width)
        out_ref[i * frames : (i + 1) * frames, :] = kept_ref[:, some] + come_ref[:, some]


def merge(kept, half, come):
    frames, columns = come.shape
    return call(
        merge_body,
        grid=(1,),
        out_shape=jax.ShapeDtypeStruct((2 * frames, columns // 2), F32),
        in_specs=[
            pl.BlockSpec((frames, columns), lambda i: (0, half)),
            pl.BlockSpec((frames, columns), lambda i: (0, 0)),
        ],
        out_specs=pl.BlockSpec((2 * frames, columns // 2), lambda i: (0, 0)),
        cost_estimate=cost(0, 12 * frames * columns),
        name="merge",
    )(kept, come)


def project_body(n_parts, n_flat, spots, n_weights, first, with_acc, with_stats, with_params, cols_ref, place_ref, *refs):
    del cols_ref

    def take(n):
        nonlocal refs
        some, refs = refs[:n], refs[n:]
        return some

    parts, flat_parts, weights = take(n_parts), take(n_flat), take(n_weights)
    acc, valid, stats_in, params = take(with_acc), take(with_stats > 0), take(with_stats > 1), take(with_params)
    (out_ref,) = take(1)
    stats, flat = take(with_stats > 0), take(n_flat > 0)
    x_high, x_low, far_ref = refs
    step = pl.program_id(0)
    width = x_high.shape[2]

    @pl.when(step == 0)
    def _():
        for block, part in zip(spots, parts):
            for start in range(0, part.shape[1], width):
                high, low = split(part[:, start : start + width])
                x_high[block + start // width] = high
                x_low[block + start // width] = low
        column = 0
        for part in flat_parts:
            flat[0][:, column : column + part.shape[1]] = part[...]
            column += part.shape[1]
        if with_acc:
            out_ref[...] = acc[0][...]
        else:
            out_ref[...] = jnp.zeros_like(out_ref)

    stacked = jnp.concatenate([x_high[step], x_low[step], x_high[step]], axis=1)
    for block, weight in enumerate(weight_blocks(place_ref, weights, far_ref)):
        w_high, w_low = split(weight)
        columns = slice(block * width, (block + 1) * width)
        out_ref[:, columns] += dot(stacked, jnp.concatenate([w_high, w_high, w_low], axis=1), NT)

    if with_stats:
        (stats_ref,) = stats

        @pl.when(step == pl.num_programs(0) - 1)
        def _():
            if stats_in:
                stats_ref[...] = stats_in[0][...]
            own = jnp.sum(valid[0][...], axis=0, keepdims=True)
            per = width // LANES
            for row in range(out_ref.shape[1] // LANES):
                z = out_ref[:, row * LANES : (row + 1) * LANES]
                total = jnp.sum(valid[0][...] * z, axis=0, keepdims=True)
                centred = valid[0][...] * (z - total / own)
                squares = jnp.sum(centred * centred, axis=0, keepdims=True)
                at = place_ref[first + row // per] * per + row % per
                stats_ref[0, pl.ds(at, 1), :] = total
                stats_ref[1, pl.ds(at, 1), :] = squares
                stats_ref[2, pl.ds(at, 1), :] = own
            if with_params:
                rest = params[0].shape[0] - 8
                stats_ref[3] = params[0][:8, :]
                stats_ref[4] = jnp.zeros_like(stats_ref[4])
                stats_ref[4, :rest, :] = params[0][8:, :]


def weight_specs(weights, layer, pairs=2):
    specs = []
    for weight in weights:
        if weight.ndim == 3:
            shape = (1, weight.shape[1], pairs * weight.shape[1])
            specs.append(pl.BlockSpec(shape, lambda s, cols, *_: (layer, 0, cols[s])))
        else:
            shape = (weight.shape[0], pairs * 4 * weight.shape[0])
            specs.append(pl.BlockSpec(shape, lambda s, cols, *_: (0, cols[s])))
    return specs


def far_scratch(width, pairs=2):
    return pltpu.VMEM((2, width, pairs * width), F32)


def weight_blocks(place_ref, refs, far_ref):
    near = [ref[0] for ref in refs if len(ref.shape) == 3]
    pieces = [ref for ref in refs if len(ref.shape) == 2]
    far = []
    for i in range(len(pieces) // 4):
        for rel, piece in enumerate(pieces[4 * i : 4 * i + 4]):
            rows = piece.shape[0]
            row = 2 * (place_ref[4] ^ (rel // 2)) + (place_ref[5] ^ (rel % 2))
            far_ref[i, pl.ds(pl.multiple_of(row * rows, rows), rows), :] = piece[...]
        far.append(far_ref[i])
    return near + far


def project(
    place, frames, parts, blocks, weights, layer, acc=None, valid=None, stats=None, params=None, flat=()
):
    near = weights[0].ndim == 3
    units = sum(1 if w.ndim == 3 else 0.25 for w in weights)
    width = weights[0].shape[1] if near else 4 * weights[0].shape[0]
    n = blocks.shape[0]
    spots, block = [], 0
    for array, _ in parts:
        spots.append(block)
        block += array.shape[1] // width
    full = pl.BlockSpec(memory_space=pltpu.VMEM)
    in_specs = [part_spec(part, frames) for part in (*parts, *flat)]
    in_specs += weight_specs(weights, layer, 1)
    operands = arrays_of(parts) + arrays_of(flat) + [in_hbm(w) for w in weights]
    array = jax.ShapeDtypeStruct((frames, int(units) * width), F32)
    array_spec = pl.BlockSpec(array.shape, lambda s, cols, place: (0, 0))
    out_shape, out_specs = [array], [array_spec]
    if acc is not None:
        in_specs.append(array_spec)
        operands.append(in_hbm(acc))
    if valid is not None:
        in_specs.append(full)
        operands.append(valid)
        shape = (3 if params is None else 5, 4 * width // LANES, LANES)
        out_shape.append(jax.ShapeDtypeStruct(shape, F32))
        out_specs.append(pl.BlockSpec(shape, lambda s, cols, place: (0, 0, 0)))
    for extra in (stats, params):
        if extra is not None:
            in_specs.append(full)
            operands.append(extra)
    if flat:
        out_shape.append(jax.ShapeDtypeStruct((frames, 4 * width), F32))
        out_specs.append(pl.BlockSpec((frames, 4 * width), lambda s, cols, place: (0, 0)))
    return call(
        partial(
            project_body,
            len(parts),
            len(flat),
            spots,
            len(weights),
            0 if near else 2,
            acc is not None,
            (valid is not None) + (stats is not None),
            params is not None,
        ),
        grid_spec=pltpu.PrefetchScalarGridSpec(
            num_scalar_prefetch=2,
            grid=(n,),
            in_specs=in_specs,
            out_specs=out_specs,
            scratch_shapes=[pltpu.VMEM((n, frames, width), BF16)] * 2 + [far_scratch(width, 1)],
        ),
        out_shape=out_shape,
        hbm_outs=(0, len(out_shape) - 1) if flat else (0,),
        cost_estimate=cost(6 * frames * n * width * units * width, 4 * n * width * units * width),
        name="project",
    )(blocks, place, *operands)


def to_relative(place_ref, spread, rows_ref, value, slot):
    per = value.shape[0] // 4
    spread[...] = value
    for rel in range(4):
        first = place_ref[rel] * per
        for row in range(per):
            rows_ref[slot, rel * per + row : rel * per + row + 1, :] = spread[
                pl.ds(first + row, 1), :
            ]


def tree(values):
    while len(values) > 1:
        values = [a + b for a, b in zip(values[::2], values[1::2])]
    return values[0]


def gathered(ref, slot):
    return [ref[i] for i in range(slot, ref.shape[0], ref.shape[0] // 16)]


def norm_terms(stats_ref):
    each = [gathered(stats_ref, slot) for slot in range(3)]
    totals, squares, owns = each
    count = tree(owns)
    mean = tree(totals) / count
    away = [total / own - mean for total, own in zip(totals, owns)]
    spread = tree([s + n * a * a for s, n, a in zip(squares, owns, away)])
    return count, mean, lax.rsqrt(spread / count + EPS)


CHUNKS = 4


def columns_of(refs, row):
    for ref in refs:
        if row * LANES < ref.shape[1]:
            return ref[:, row * LANES : (row + 1) * LANES]
        row -= ref.shape[1] // LANES


def recur_body(n_z, last, layer, spread_params, place_ref, gate_ref, *refs):
    z_refs, refs = refs[:n_z], refs[n_z:]
    (stats_ref, params_ref, valid_ref, x_ref), refs = refs[:4], refs[4:]
    outs, refs = refs[: 1 + 3 * last], refs[1 + 3 * last :]
    if spread_params:
        state_ref, slope_ref, params_out, rows, spread, held, drive_s, state_s, slope_s = refs
    else:
        state_ref, slope_ref, rows, spread, held, drive_s, state_s, slope_s = refs
    frames, features = x_ref.shape
    blocks = features // LANES
    per = blocks // 4
    chunk = pl.program_id(0)

    @pl.when(chunk == 0)
    def _():
        if spread_params:
            for rel in range(4):
                first = place_ref[rel] * (stats_ref.shape[0] // 16) + 3
                for row in range(LAYERS * 3 * per):
                    at = rel * per + row % per
                    params_out[row // per, at : at + 1, :] = stats_ref[
                        first + row // 8, row % 8 : row % 8 + 1, :
                    ]
            params = [params_out[3 * layer + i] for i in range(3)]
        else:
            params = [params_ref[3 * layer + i] for i in range(3)]
        _, mean, inv_std = norm_terms(stats_ref)
        to_relative(place_ref, spread, rows, mean, 0)
        to_relative(place_ref, spread, rows, inv_std, 1)
        rows[1] = rows[1] * params[0]
        rows[2] = params[1]
        rows[3] = params[2]
        held[...] = jnp.zeros_like(held)

    for row in range(blocks):
        drive_s[row * frames : (row + 1) * frames, :] = (
            columns_of(z_refs, row) - rows[0, row : row + 1, :]
        ) * rows[1, row : row + 1, :] + rows[2, row : row + 1, :]
    decay = rows[3]

    def step(t, state):
        at = pl.ds(t, blocks, stride=frames)
        pre = drive_s[at, :] + decay * state
        half = 0.5 + 0.5 * lax.erf(pre * (1.0 / ROOT_TWO))
        gate = gate_ref[chunk * frames + t] > 0.0
        slope = half + pre * jnp.exp(-0.5 * pre * pre) * (1.0 / ROOT_TWO_PI)
        state = jnp.where(gate, pre * half, state)
        state_s[at, :] = state
        slope_s[at, :] = jnp.where(gate, slope, 0.0)
        return state

    held[...] = lax.fori_loop(0, frames, step, held[...], unroll=8)
    valid = valid_ref[...]
    for row in range(blocks):
        lanes = slice(row * LANES, (row + 1) * LANES)
        state = state_s[row * frames : (row + 1) * frames, :]
        state_ref[:, lanes] = state
        slope_ref[:, lanes] = slope_s[row * frames : (row + 1) * frames, :]
        value = x_ref[:, lanes] + valid * state
        out, at = (outs[row // per], row % per) if last else (outs[0], row)
        out[:, at * LANES : (at + 1) * LANES] = value


def recur(layer, place, gate, z, stats, params, valid, x, last):
    frames, features = x.shape
    blocks = features // LANES
    some = frames // CHUNKS
    whole = lambda array: pl.BlockSpec(array.shape, lambda i: (0,) * array.ndim)
    by_chunk = lambda array: pl.BlockSpec((some, array.shape[1]), lambda i: (i, 0))
    full = jax.ShapeDtypeStruct((frames, features), F32)
    piece = jax.ShapeDtypeStruct((frames, features // 4), F32)
    out_shape = [piece] * 4 if last else [full]
    out_shape += [full, full]
    out_specs = [by_chunk(a) for a in out_shape]
    spread_params = params is None
    if spread_params:
        out_shape.append(jax.ShapeDtypeStruct((3 * LAYERS, blocks, LANES), F32))
        out_specs.append(whole(out_shape[-1]))
        params = valid
    return call(
        partial(recur_body, len(z), last, layer, spread_params),
        grid=(CHUNKS,),
        in_specs=[SMEM_SPEC, SMEM_SPEC]
        + [by_chunk(a) for a in z]
        + [whole(a) for a in (stats, params)]
        + [by_chunk(a) for a in (valid, x)],
        out_specs=out_specs,
        out_shape=out_shape,
        hbm_outs=tuple(range(len(out_shape) - spread_params)) if last else (1, 2),
        scratch_shapes=[
            pltpu.VMEM((4, blocks, LANES), F32),
            pltpu.VMEM((blocks, LANES), F32),
            pltpu.VMEM((blocks, LANES), F32),
        ]
        + [pltpu.VMEM((blocks * some, LANES), F32)] * 3,
        cost_estimate=cost(100 * frames * features, 20 * frames * features),
        name="recur",
    )(place, gate, *[in_hbm(a) for a in z], stats, params, valid, in_hbm(x))


def back_body(n_z, n_ups, spots, layer, place_ref, gate_ref, *refs):
    z_refs, refs = refs[:n_z], refs[n_z:]
    (stats_ref, params_ref), refs = refs[:2], refs[2:]
    ups, (state_ref, slope_ref), refs = refs[:n_ups], refs[n_ups : n_ups + 2], refs[n_ups + 2 :]
    grad_ref, sums_ref, rows, spread, held, up_s, state_s, slope_s = refs
    frames, features = state_ref.shape
    blocks = features // LANES
    per = blocks // 4
    tall = frames + 8
    step_no = pl.program_id(0)
    chunk = pl.num_programs(0) - 1 - step_no

    @pl.when(step_no == 0)
    def _():
        _, mean, inv_std = norm_terms(stats_ref)
        to_relative(place_ref, spread, rows, mean, 0)
        to_relative(place_ref, spread, rows, inv_std, 1)
        held[...] = jnp.zeros_like(held)

    for row in range(blocks):
        lanes = slice(row * LANES, (row + 1) * LANES)
        base = row * frames
        up = None
        for (_, column), part in zip(spots, ups):
            if column <= row * LANES < column + part.shape[1]:
                value = part[:, row * LANES - column : (row + 1) * LANES - column]
                up = value if up is None else up + value
        up_s[base : base + frames, :] = up
        state_s[row * tall : row * tall + 8, :] = jnp.zeros((8, LANES), F32)
        state_s[row * tall + 8 : (row + 1) * tall, :] = state_ref[:, lanes]
        slope_s[base : base + frames, :] = slope_ref[:, lanes]
    decay = params_ref[3 * layer + 2]

    def step(i, carry):
        t = frames - 1 - i
        at = pl.ds(t, blocks, stride=frames)
        slope = slope_s[at, :]
        gate = gate_ref[chunk * frames + t]
        total = gate * up_s[at, :] + carry
        up_s[at, :] = total * slope
        return total * (slope * decay + (1.0 - gate))

    held[0] = lax.fori_loop(0, frames, step, held[0], unroll=8)
    held[4] += held[1] * state_s[pl.ds(tall - 1, blocks, stride=tall), :]
    held[1] = up_s[pl.ds(0, blocks, stride=frames), :]
    for row in range(blocks):
        lanes = slice(row * LANES, (row + 1) * LANES)
        grad = up_s[row * frames : (row + 1) * frames, :]
        grad_ref[:, lanes] = grad
        zhat = (columns_of(z_refs, row) - rows[0, row : row + 1, :]) * rows[1, row : row + 1, :]
        before = state_s[row * tall + 7 : row * tall + 7 + frames, :]
        for slot, value in enumerate((grad * zhat, grad, grad * before)):
            held[2 + slot, row : row + 1, :] += jnp.sum(value, axis=0, keepdims=True)

    @pl.when(chunk == 0)
    def _():
        for row in range(blocks):
            at = place_ref[row // per] * per + row % per
            for slot in range(3):
                sums_ref[slot, pl.ds(at, 1), :] = held[2 + slot, row : row + 1, :]


def spots_of_sum(parts, width):
    spots, column = [], 0
    for array, _ in parts:
        spots.append((0, column % (4 * width)))
        column += array.shape[1]
    return spots


def back(layer, place, gate, z, stats, params, ups, states, slopes):
    frames, features = states.shape
    width = features // 4
    blocks = features // LANES
    some = frames // CHUNKS
    whole = lambda array: pl.BlockSpec(array.shape, lambda i: (0,) * array.ndim)

    def by_chunk(array, first=0):
        return pl.BlockSpec(
            (some, array.shape[1]), lambda i: ((first or 0) * CHUNKS + CHUNKS - 1 - i, 0)
        )

    out_shape = [
        jax.ShapeDtypeStruct((frames, features), F32),
        jax.ShapeDtypeStruct((3, blocks, LANES), F32),
    ]
    return call(
        partial(back_body, len(z), len(ups), spots_of_sum(ups, width), layer),
        grid=(CHUNKS,),
        in_specs=[SMEM_SPEC] * 2
        + [by_chunk(a) for a in z]
        + [whole(a) for a in (stats, params)]
        + [by_chunk(*up) for up in ups]
        + [by_chunk(a) for a in (states, slopes)],
        out_specs=[by_chunk(out_shape[0]), whole(out_shape[1])],
        out_shape=out_shape,
        scratch_shapes=[
            pltpu.VMEM((2, blocks, LANES), F32),
            pltpu.VMEM((blocks, LANES), F32),
            pltpu.VMEM((5, blocks, LANES), F32),
            pltpu.VMEM((blocks * some, LANES), F32),
            pltpu.VMEM((blocks * (some + 8), LANES), F32),
            pltpu.VMEM((blocks * some, LANES), F32),
        ],
        cost_estimate=cost(30 * frames * features, 20 * frames * features),
        name="back",
    )(
        place,
        gate,
        *[in_hbm(a) for a in z],
        stats,
        params,
        *arrays_of(ups),
        in_hbm(states),
        in_hbm(slopes),
    )


def input_terms(high_s, low_s, weights):
    left, right = [], []
    for block, weight in enumerate(weights):
        w_high, w_low = split(weight)
        left += [high_s[block], low_s[block], high_s[block]]
        right += [w_high, w_high, w_low]
    return dot(jnp.concatenate(left, axis=1), jnp.concatenate(right, axis=0), NN)


def norm_back_body(n_z, split_terms, layer, cols_ref, place_ref, grad_ref, *refs):
    del cols_ref
    z_refs, refs = refs[:n_z], refs[n_z:]
    params_ref, valid_ref, stats_ref, sums_ref, *refs = refs
    weights, refs = refs[:10], refs[10:]
    if split_terms:
        out_ref, leave_ref, near_term_ref, far_term_ref, sums_out_ref, *refs = refs
        term_refs, starts = (far_term_ref, near_term_ref), (0, 0)
    else:
        out_ref, leave_ref, term_ref, sums_out_ref, *refs = refs
        term_refs, starts = (term_ref, term_ref), (2 * grad_ref.shape[1] // 4, 0)
    rows, spread, high_s, low_s, far_ref = refs
    blocks = grad_ref.shape[1] // LANES
    width = high_s.shape[2]
    per = width // LANES

    @pl.when(pl.program_id(0) == 0)
    def _():
        count, mean, inv_std = norm_terms(stats_ref)
        to_relative(place_ref, spread, rows, mean, 0)
        to_relative(place_ref, spread, rows, inv_std, 1)
        rows[2] = rows[1] * params_ref[3 * layer]
        sums = [tree(gathered(sums_ref, slot)) for slot in range(3)]
        for slot in range(3):
            sums_out_ref[slot] = sums[slot]
        to_relative(place_ref, spread, rows, sums[0] / count, 3)
        to_relative(place_ref, spread, rows, sums[1] / count, 4)
        valid = valid_ref[...]
        for row in range(blocks):
            lanes = slice(row * LANES, (row + 1) * LANES)
            one = lambda slot: rows[slot, row : row + 1, :]
            zhat = (columns_of(z_refs, row) - one(0)) * one(1)
            value = one(2) * (grad_ref[:, lanes] - valid * (one(4) + zhat * one(3)))
            out_ref[:, lanes] = value
            if (row // per) % 2:
                at = (row // per // 2) * width + (row % per) * LANES
                leave_ref[:, at : at + LANES] = value
            high, low = split(value)
            inner = slice((row % per) * LANES, (row % per + 1) * LANES)
            high_s[row // per, :, inner] = high
            low_s[row // per, :, inner] = low

    value = input_terms(high_s, low_s, weight_blocks(place_ref, weights, far_ref))
    for step, (term_ref, first) in enumerate(zip(term_refs, starts)):

        @pl.when(pl.program_id(0) == step)
        def _():
            for pair in range(2):
                at = pl.multiple_of(((place_ref[0] & 1) ^ pair) * width, width)
                term_ref[:, pl.ds(first + at, width)] = value[
                    :, pair * width : (pair + 1) * width
                ]


def norm_back(columns, place, grad, z, params, valid, stats, sums, weights, layer, split_terms):
    frames, features = grad.shape
    width = features // 4
    blocks = features // LANES
    whole = lambda array: pl.BlockSpec(array.shape, lambda s, cols, place: (0,) * array.ndim)
    operands = [grad, *[in_hbm(a) for a in z], params, valid, stats, sums]
    full = jax.ShapeDtypeStruct((frames, features), F32)
    half = jax.ShapeDtypeStruct((frames, 2 * width), F32)
    terms = [half, half] if split_terms else [full]
    out_shape = [full, half, *terms, jax.ShapeDtypeStruct((3, blocks, LANES), F32)]
    return call(
        partial(norm_back_body, len(z), split_terms, layer),
        grid_spec=pltpu.PrefetchScalarGridSpec(
            num_scalar_prefetch=2,
            grid=(2,),
            in_specs=[whole(a) for a in operands] + weight_specs(weights, layer),
            out_specs=[whole(a) for a in out_shape],
            scratch_shapes=[
                pltpu.VMEM((5, blocks, LANES), F32),
                pltpu.VMEM((blocks, LANES), F32),
                pltpu.VMEM((4, frames, width), BF16),
                pltpu.VMEM((4, frames, width), BF16),
                far_scratch(width),
            ],
        ),
        out_shape=out_shape,
        hbm_outs=(0,),
        cost_estimate=cost(6 * frames * features * features, 4 * features * features),
        name="norm_back",
    )(columns, place, *operands, *[in_hbm(w) for w in weights])


def own_terms_body(n_ups, spots, cols_ref, place_ref, grad_ref, *refs):
    del cols_ref
    ups, refs = refs[:n_ups], refs[n_ups:]
    weights, refs = refs[:10], refs[10:]
    out_ref, high_s, low_s, far_ref = refs
    width = high_s.shape[2]
    step = pl.program_id(0)

    @pl.when(step == 0)
    def _():
        for block in range(4):
            high, low = split(grad_ref[:, block * width : (block + 1) * width])
            high_s[block] = high
            low_s[block] = low

    value = input_terms(high_s, low_s, weight_blocks(place_ref, weights, far_ref))
    for pair in range(2):
        at = pl.multiple_of(((place_ref[0] & 1) ^ pair) * width, width)
        out_ref[:, pl.ds(at, width)] = value[:, pair * width : (pair + 1) * width]
    for half in range(2):

        @pl.when(step == half)
        def _():
            first = 2 * half * width
            for (_, column), up in zip(spots, ups):
                low = max(column, first)
                high = min(column + up.shape[1], first + 2 * width)
                if low < high:
                    out_ref[:, low - first : high - first] += up[:, low - column : high - column]


def own_terms(columns, place, grad, ups, weights, layer):
    frames, features = grad.shape
    width = features // 4
    whole = lambda array: pl.BlockSpec(array.shape, lambda s, cols, place: (0,) * array.ndim)
    step_block = pl.BlockSpec((frames, 2 * width), lambda s, cols, place: (0, s))
    return call(
        partial(own_terms_body, len(ups), spots_of_sum(ups, width)),
        grid_spec=pltpu.PrefetchScalarGridSpec(
            num_scalar_prefetch=2,
            grid=(2,),
            in_specs=[whole(grad)]
            + [part_spec(up, frames) for up in ups]
            + weight_specs(weights, layer),
            out_specs=step_block,
            scratch_shapes=[pltpu.VMEM((4, frames, width), BF16)] * 2 + [far_scratch(width)],
        ),
        out_shape=jax.ShapeDtypeStruct((frames, features), F32),
        cost_estimate=cost(6 * frames * features * features, 4 * features * features),
        name="own_terms",
    )(columns, place, in_hbm(grad), *arrays_of(ups), *[in_hbm(w) for w in weights])


def prepare_body(n_chunks, lists_ref, place_ref, *refs):
    del lists_ref
    groups = []
    for _ in range(4):
        groups.append(refs[:n_chunks])
        refs = refs[n_chunks:]
    high_ref, low_ref = refs
    padded = high_ref.shape[0] // 2
    width = high_ref.shape[1] // 2
    for side in range(2):

        @pl.when(pl.program_id(0) // 2 == side)
        def _():
            for clip in range(2):
                for dc in range(2):
                    at = pl.multiple_of((place_ref[6] ^ clip ^ dc) * width, width)
                    row = clip * padded
                    for part in groups[2 * clip + side]:
                        rows = part.shape[0]
                        high, low = split(part[:, dc * width : (dc + 1) * width])
                        high_ref[row : row + rows, pl.ds(at, width)] = high
                        low_ref[row : row + rows, pl.ds(at, width)] = low
                        row += rows
                rest = (clip + 1) * padded - row
                zeros = jnp.zeros((rest, 2 * width), BF16)
                high_ref[row : row + rest, :] = zeros
                low_ref[row : row + rest, :] = zeros


def prepare(lists, place, groups):
    width = groups[0][0].shape[1] // 4
    frames = sum(part.shape[0] for part in groups[0])
    padded = -(-frames // LANES) * LANES
    in_specs = []
    for i, group in enumerate(groups):
        for part in group:
            if i % 2 == 0:
                index = lambda s, *_: (0, jnp.minimum(s, 1))
            else:
                index = lambda s, *_: (0, jnp.maximum(s - 2, 0))
            in_specs.append(pl.BlockSpec((part.shape[0], 2 * width), index))
    out = jax.ShapeDtypeStruct((2 * padded, 8 * width), BF16)
    out_spec = pl.BlockSpec((2 * padded, 2 * width), lambda s, cols, place: (0, cols[s]))
    return call(
        partial(prepare_body, len(groups[0])),
        grid_spec=pltpu.PrefetchScalarGridSpec(
            num_scalar_prefetch=2,
            grid=(4,),
            in_specs=in_specs,
            out_specs=[out_spec, out_spec],
        ),
        out_shape=[out, out],
        hbm_outs=(0, 1),
        cost_estimate=cost(0, 16 * frames * 8 * width),
        name="prepare",
    )(lists, place, *[in_hbm(part) for group in groups for part in group])


def product(g_high, g_low, x_high, x_low):
    return dot(g_high, x_high, NN) + (dot(g_high, x_low, NN) + dot(g_low, x_high, NN))


def weight_body(turn, place_ref, *refs):
    if turn:
        grad_ref, near_ref, x_high, x_low, kept, sent, g_high, g_low, t_high, t_low = refs

        @pl.when(pl.program_id(0) == 0)
        def _():
            frames, features = grad_ref.shape
            width = features // 4
            rows = width // 4
            padded = t_high.shape[1] // 2
            t_high[...] = jnp.zeros_like(t_high)
            t_low[...] = jnp.zeros_like(t_low)
            for clip in range(2):
                for dh in range(2):
                    if clip == 0:
                        part = grad_ref[:, 2 * dh * width : (2 * dh + 1) * width]
                    else:
                        part = near_ref[:, dh * width : (dh + 1) * width]
                    high, low = split(part.T)
                    at = (
                        slice(dh * width, (dh + 1) * width),
                        slice(clip * padded, clip * padded + frames),
                    )
                    t_high[at] = high
                    t_low[at] = low
            for group in range(8):
                first, second, dh = group // 4, group // 2 % 2, group % 2
                core = place_ref[6]
                y = place_ref[4] ^ (first * core + second * (1 - core))
                x = place_ref[5] ^ (first * (1 - core) + second * core)
                at = pl.multiple_of(dh * width + (2 * y + x) * rows, rows)
                g_high[group * rows : (group + 1) * rows, :] = t_high[pl.ds(at, rows), :]
                g_low[group * rows : (group + 1) * rows, :] = t_low[pl.ds(at, rows), :]

    else:
        g_high, g_low, x_high, x_low, kept, sent = refs
    half = g_high.shape[0] // 2
    value = product(g_high[...], g_low[...], x_high[...], x_low[...])
    kept[...] = value[:half].reshape(kept.shape)
    sent[...] = value[half:].reshape(sent.shape)


def weight_rows(half, place, grads, x_split, width):
    turn = half == 0
    whole = lambda array: pl.BlockSpec(array.shape, lambda s, place: (0,) * array.ndim)
    x_spec = pl.BlockSpec((x_split[0].shape[0], width), lambda s, place: (0, 4 * half + s))
    shape = (2, 2, width // 4, 4 * width)
    out_shape = [jax.ShapeDtypeStruct(shape, F32)] * 2
    out_specs = [pl.BlockSpec(shape[:3] + (width,), lambda s, place: (0, 0, 0, s))] * 2
    scratch = []
    if turn:
        turned = (2 * width, x_split[0].shape[0])
        out_shape += [jax.ShapeDtypeStruct(turned, BF16)] * 2
        out_specs += [whole(out_shape[-1])] * 2
        scratch = [pltpu.VMEM(turned, BF16)] * 2
    return call(
        partial(weight_body, turn),
        grid_spec=pltpu.PrefetchScalarGridSpec(
            num_scalar_prefetch=1,
            grid=(4,),
            in_specs=[whole(a) for a in grads] + [x_spec] * 2,
            out_specs=out_specs,
            scratch_shapes=scratch,
        ),
        out_shape=out_shape,
        hbm_outs=(0,),
        cost_estimate=cost(12 * x_split[0].shape[0] * width * 4 * width, 4 * 8 * width * width),
        name="weight_rows",
    )(place, *([in_hbm(grads[0]), grads[1]] if turn else grads), *[in_hbm(x) for x in x_split])


def step_body(n, widths, cut, *refs):
    ins, outs = refs[: 2 * n], refs[2 * n :]
    starts = [sum(widths[:i]) for i in range(len(widths))]
    column = 0
    for i in range(n):
        total = ins[2 * i][...] + ins[2 * i + 1][...]
        end = column + total.shape[-1]
        for j, (start, columns) in enumerate(zip(starts, widths)):
            low, high = max(start, column), min(start + columns, end)
            if low < high:
                to = (Ellipsis, slice(low - start, high - start))
                piece = total[..., low - column : high - column]
                if cut:
                    outs[2 * j][to] = piece[0]
                    outs[2 * j + 1][to] = piece[1]
                else:
                    outs[j][to] = piece
        column = end


def step_of(*pairs, cut=True, widths=None):
    shape = list(pairs[0][0].shape)
    widths = widths or [sum(pair[0].shape[-1] for pair in pairs)]
    outs = []
    for columns in widths:
        shape[-1] = columns
        out = jax.ShapeDtypeStruct(tuple(shape[1:] if cut else shape), F32)
        outs += [out] * (1 + cut)
    whole = lambda array: pl.BlockSpec(array.shape, lambda i: (0,) * array.ndim)
    operands = [array for pair in pairs for array in pair]
    return call(
        partial(step_body, len(pairs), widths, cut),
        grid=(1,),
        in_specs=[whole(a) for a in operands],
        out_specs=[whole(a) for a in outs],
        out_shape=outs,
        cost_estimate=cost(0, 4 * sum(a.size for a in operands)),
        name="reduction_step",
    )(*operands)


def plane_swap(array, step):
    pairs = []
    for i in range(8):
        over_x = (i % 2 == 0) == (step == 0)
        pairs.append((i, i ^ 2 if over_x else i ^ 4))
    return lax.ppermute(array, ("y", "x", "c"), pairs)


def plane_gather(share, *before):
    first = plane_swap(share, 0)
    second = plane_swap(share, 1)
    return [share, second, first, plane_swap(after(first, *before), 1)]


def assemble_body(groups, place_ref, *refs):
    out_ref = refs[-1]
    core = place_ref[6]
    column = 0
    for group in range(groups):
        rows, columns = refs[4 * group].shape
        for i in range(4):
            first, second = i // 2, i % 2
            y = place_ref[4] ^ (first * core + second * (1 - core))
            x = place_ref[5] ^ (first * (1 - core) + second * core)
            at = pl.multiple_of((2 * y + x) * rows, rows)
            out_ref[0, pl.ds(at, rows), column : column + columns] = refs[4 * group + i][...]
        column += columns


def assemble(place, groups, layer, onto=None):
    pieces = [piece for group in groups for piece in group]
    rows = 4 * pieces[0].shape[0]
    columns = sum(group[0].shape[1] for group in groups)
    aliases, extra, extra_specs = {}, [], []
    if onto is not None:
        aliases, extra = {1 + len(pieces): 0}, [onto]
        extra_specs = [pl.BlockSpec(memory_space=pl.ANY)]
    (out,) = call(
        partial(assemble_body, len(groups)),
        grid=(1,),
        out_shape=[jax.ShapeDtypeStruct((LAYERS, rows, columns), F32)],
        hbm_outs=(0,),
        in_specs=[SMEM_SPEC]
        + [pl.BlockSpec(p.shape, lambda i: (0, 0)) for p in pieces]
        + extra_specs,
        out_specs=[pl.BlockSpec((1, rows, columns), lambda i: (layer, 0, 0))],
        input_output_aliases=aliases,
        cost_estimate=cost(0, 8 * rows * columns),
        name="assemble",
    )(place, *[p if extra else in_hbm(p) for p in pieces], *extra)
    return out


def half_features(inputs, weights, gains, shifts, decays, biases, lengths, frame_mask, grad_out):
    width, slots = inputs.shape
    clips, frames = frame_mask.shape
    depth = weights.shape[2]
    blocks = 4 * width // LANES
    y, x, h, l, c = (lax.axis_index(name) for name in ("y", "x", "h", "l", "c"))
    b = 2 * y + x
    numbers = [2 * (h ^ (rel // 2)) + (c ^ (rel % 2)) for rel in range(4)] + [y, x, c]
    place = jnp.stack(numbers).astype(jnp.int32)
    own_blocks, other_blocks = (
        jnp.stack(
            [2 * (2 * (h ^ (rel // 2)) + half) + (c ^ (rel % 2)) for rel in range(4)]
        ).astype(jnp.int32)
        for half in (l, 1 - l)
    )
    own_columns = jnp.stack([2 * h + l, 2 * (1 - h) + l]).astype(jnp.int32)
    other_columns = jnp.stack([2 * (1 - h) + 1 - l, 2 * h + 1 - l]).astype(jnp.int32)
    all_columns = jnp.concatenate([own_columns, other_columns[::-1]])
    rows = width // 4

    clip = 2 * h + c
    seen = lax.dynamic_index_in_dim(frame_mask, clip, 0, keepdims=False)
    length = lax.dynamic_index_in_dim(lengths, clip, 0, keepdims=False)
    moments = jnp.arange(frames, dtype=jnp.int32)
    gate = ((moments < length) & ((seen == 1) | (moments == 0))).astype(F32)
    valid = jnp.broadcast_to(gate[:, None], (frames, LANES))

    def far_share(layer):
        return lax.dynamic_slice(weights, (layer, b * rows, 0), (1, rows, depth))[0]

    def over_h(array):
        return lax.ppermute(array, "h", FLIP2)

    def over_c(array):
        return lax.ppermute(array, "c", FLIP2)

    def over_second(array):
        return plane_swap(array, 1)

    def four_of(near_rows, far_rows):
        return [
            (near_rows, 0),
            (over_c(near_rows), 1),
            (far_rows, 0),
            (over_c(far_rows), 1),
        ]

    def far_pieces(share):
        both = lax.ppermute(share, ("y", "x"), DIAGONAL)
        return [share, lax.ppermute(share, "x", FLIP2), lax.ppermute(share, "y", FLIP2), both]

    near = over_c(weights)
    share = far_share(0)
    close, away = pack(place, after(inputs, share), frames)
    share = over_h(share)
    away = over_h(away)
    other_close = swap_half(close)
    up_close, up_away = pack(place, after(grad_out, close), frames, waits=True)
    share = after(share, up_close, valid, near, other_close)
    pieces = far_pieces(share)
    away = after(away, pieces[1:])
    half_weights = [[weights, near, *pieces, *map(over_c, after(pieces, away))]]
    own = four_of(after(close, away), away)
    other_away = swap_half(away)
    others = [(other_close, 0), (over_c(other_close), 1)]
    params = jnp.stack([gains, shifts + biases, decays], axis=1)
    own_params = params.reshape(LAYERS * 3 * width // LANES, LANES)
    params = None

    def gather(array, axes):
        return lax.all_gather(array, axes, tiled=True)

    weight = half_weights[0]
    early = jnp.concatenate([own_blocks, other_blocks[:2]])
    z, own_flat = project(place, frames, own + others, early, weight, 0, flat=own)
    others += [(other_away, 0), (over_c(after(other_away, z)), 1)]
    z, stats, other_flat = project(
        place,
        frames,
        others[2:],
        other_blocks[2:],
        weight,
        0,
        z,
        valid,
        params=own_params,
        flat=others,
    )
    z = [z]
    stats = gather(stats, ("h", "c"))
    share = over_c(lax.ppermute(after(far_share(1), stats), ("h", "c"), DIAGONAL))
    stats = gather(stats, ("y", "x"))
    x, states, slopes, params = recur(0, place, gate, z, stats, None, valid, own_flat, False)
    groups = [[own_flat], [other_flat]]
    groups += [[over_c(after(p, z[0])) for p in group] for group in groups]
    x_split = prepare(all_columns, place, after(groups, slopes))
    saved = [(groups, x_split, z, stats, states, slopes)]

    pieces = far_pieces(after(share, slopes, groups))
    near = [weights, near]
    other = swap_half(x)
    z, *_ = project(place, frames, [(after(x, x_split[0]), None)], own_blocks, near, 1)
    far = [*pieces, *map(over_c, after(pieces, z))]
    up_away = over_h(after(up_away, other, z))
    half_weights.append(near + far)
    z, stats = project(place, frames, [(other, None)], other_blocks, near, 1, z, valid)
    both = jnp.concatenate([own_blocks, other_blocks])
    z_far, stats = project(
        place,
        frames,
        [(x, None), (other, None)],
        both,
        far,
        1,
        None,
        valid,
        stats,
    )
    z = [z, z_far]
    stats = gather(gather(stats, ("y", "x")), ("h", "c"))
    upstream = four_of(up_close, after(up_away, stats))
    *output, states, slopes = recur(1, place, gate, z, stats, params, valid, x, True)
    groups = [[x], [other]]
    groups += [[over_c(after(p, slopes)) for p in group] for group in groups]
    saved.append((groups, None, z, stats, states, slopes))
    diagonal = over_c(over_h(output[3]))

    ups = upstream
    results = [None] * LAYERS
    for layer in range(LAYERS - 1, -1, -1):
        groups, x_split, z, stats, states, slopes = saved[layer]
        weight = half_weights[layer]
        grad_pre, sums = back(layer, place, gate, z, stats, params, ups, states, slopes)
        sums = gather(sums, ("y", "x"))
        if layer == 0:
            later, go = step_of(*[(in_hbm(k), after(g, sums)) for k, g in zip(stay, come)])
            sums = after(sums, later)
            go = over_second(go)
        sums = gather(sums, ("h", "c"))
        if layer > 0:
            away = over_h(after(output[2], sums))
        grad_z, leaving, *terms, sums = norm_back(
            other_columns, place, grad_pre, z, params, valid, stats, sums, weight, layer,
            layer == 0,
        )
        leaving = over_c(leaving)
        if layer > 0:
            received = [swap_half(terms[0])]
            x_split = prepare(all_columns, place, after(groups, grad_z, diagonal))
        else:
            received = [None, swap_half(terms[1])]
            later, go = step_of((later, after(go, grad_z)))
            leaving = after(leaving, later)
            later = (later, over_h(go))
        *first, g_high, g_low = weight_rows(0, place, (grad_z, leaving), x_split, width)
        turned = (g_high, g_low)
        come = [plane_swap(first[1], 0)]
        if layer > 0:
            turned = after(turned, away)
            output = [(a, 0) for a in (output[0], over_c(output[1]), away, diagonal)]
        else:
            received[0] = swap_half(after(terms[0], received[1]))
        second = weight_rows(1, place, turned, x_split, width)
        come.append(plane_swap(second[1], 0))
        stay = (first[0], second[0])
        kept = own_terms(own_columns, place, after(grad_z, second[0]), ups, weight, layer)
        ups = [(kept, None)] + [(r, None) for r in received]
        results[layer] = lax.dynamic_index_in_dim(
            sums.reshape(3, 4, width), clip, axis=1, keepdims=False
        )

    sums = jnp.stack(results)
    sums = [sums[:, 0], sums[:, 1], sums[:, 2]]
    away = merge(kept, 1, received[1])
    (later,) = step_of((later[0], after(later[1], away)), cut=False)
    away = over_h(away)
    later_first, later_second = plane_swap(later, 0), plane_swap(later, 1)
    come[0] = after(come[0], later_first, sums)
    total, go = step_of((in_hbm(stay[0]), come[0]), (in_hbm(stay[1]), come[1]))
    go = over_second(go)
    later = [later, later_second, later_first, plane_swap(after(later_first, total), 1)]
    far = [(away, 0), (over_c(away), 1)]
    total, go = step_of((total, after(go, far[1][0])))
    go = over_h(go)
    output = unpack(place, [(after(array, total), i) for array, i in output], frames, waited=True)
    grad_weights = assemble(place, after([later], output), 1)
    close = merge(kept, 0, after(received[0], grad_weights))
    (share,) = step_of((total, after(go, close)), cut=False)
    gathered = plane_gather(share)
    grad_in = [(close, 0), (over_c(close[frames:]), 0)] + far
    grad_in = unpack(place, grad_in, frames)
    grad_weights = assemble(place, after([gathered], grad_in), 0, grad_weights)
    return (output, grad_in, grad_weights, *sums, sums[1])


def gelu_slope(value):
    return (
        0.5 * (1.0 + jax.scipy.special.erf(value / ROOT_TWO))
        + value * jnp.exp(-0.5 * value * value) / ROOT_TWO_PI
    )


def recur_step(decay, state, inputs):
    drive_t, valid_t = inputs
    pre = drive_t + decay * state
    state = state + valid_t * (jax.nn.gelu(pre, approximate=False) - state)
    return (state, state)


def back_step(decay, carry, inputs):
    upstream_t, valid_t, pre_t = inputs
    total = upstream_t + carry
    grad_pre = total * valid_t * gelu_slope(pre_t)
    carry = total * (1.0 - valid_t) + grad_pre * decay
    return (carry, grad_pre)


def add_piece(weight, piece):
    return jnp.dot(weight, piece, precision=HIGH, preferred_element_type=jnp.float32)


def weight_columns(grad_pre_norm, piece):
    return jnp.einsum("jf,kf->jk", grad_pre_norm, piece, precision=HIGH)


def split_features(inputs, weights, gains, shifts, decays, biases, lengths, frame_mask, grad_out):
    width, slots = inputs.shape
    clips, frames_len = frame_mask.shape
    frames = jnp.arange(frames_len, dtype=jnp.int32)
    valid_grid = (
        (frames[None, :] < lengths[:, None]) & ((frame_mask == 1) | (frames[None, :] == 0))
    ).astype(jnp.float32)
    valid = valid_grid.reshape(-1)
    valid_row = valid[None, :]
    valid_time = jnp.broadcast_to(valid_grid.T[:, :, None], (frames_len, clips, width)).reshape(
        frames_len, clips * width
    )
    count_local = jnp.sum(valid)

    def to_time(array):
        return jnp.transpose(array.reshape(width, clips, frames_len), (2, 1, 0)).reshape(
            frames_len, clips * width
        )

    def from_time(array):
        return jnp.transpose(array.reshape(frames_len, clips, width), (2, 1, 0)).reshape(
            width, slots
        )

    layer_in = inputs
    saved = []
    for layer_no in range(LAYERS):
        weight = weights[layer_no]
        gathered = lax.all_gather(layer_in, "neuron", axis=0, tiled=True)
        pre_norm = add_piece(weight, gathered)
        first_sum, count = lax.psum((jnp.sum(valid_row * pre_norm, axis=1), count_local), "batch")
        mean = first_sum / count
        centered = pre_norm - mean[:, None]
        var = lax.psum(jnp.sum(valid_row * centered * centered, axis=1), "batch") / count
        inv_std = lax.rsqrt(var + EPS)
        zhat = (pre_norm - mean[:, None]) * inv_std[:, None]
        drive = gains[layer_no][:, None] * zhat + (shifts[layer_no] + biases[layer_no])[:, None]
        drive_time = to_time(drive)
        decay_wide = jnp.tile(decays[layer_no], clips)
        start_state = jnp.zeros((clips * width,), jnp.float32)
        _, states = lax.scan(
            partial(recur_step, decay_wide), start_state, (drive_time, valid_time), unroll=8
        )
        saved.append((gathered, zhat, inv_std, drive_time, states, count))
        layer_in = layer_in + valid_row * from_time(states)
    upstream = grad_out
    grad_parts = [None] * LAYERS
    for layer_no in range(LAYERS - 1, -1, -1):
        gathered, zhat, inv_std, drive_time, states, count = saved[layer_no]
        decay_wide = jnp.tile(decays[layer_no], clips)
        gain = gains[layer_no]
        previous = jnp.concatenate([jnp.zeros_like(states[:1]), states[:-1]], axis=0)
        pre_time = drive_time + decay_wide[None, :] * previous
        grad_state = to_time(valid_row * upstream)
        start_carry = jnp.zeros((clips * width,), jnp.float32)
        _, grad_pre_time = lax.scan(
            partial(back_step, decay_wide),
            start_carry,
            (grad_state, valid_time, pre_time),
            reverse=True,
            unroll=8,
        )
        decay_local = jnp.sum(
            jnp.sum(grad_pre_time * previous, axis=0).reshape(clips, width), axis=0
        )
        grad_pre = from_time(grad_pre_time)
        gain_local = jnp.sum(grad_pre * zhat, axis=1)
        shift_local = jnp.sum(grad_pre, axis=1)
        grad_gain, grad_shift, grad_decay = lax.psum(
            (gain_local, shift_local, decay_local), "batch"
        )
        grad_pre_norm = (gain * inv_std)[:, None] * (
            grad_pre - valid_row * (grad_shift[:, None] + zhat * grad_gain[:, None]) / count
        )
        weight_local = weight_columns(grad_pre_norm, gathered)
        input_terms = jnp.einsum("jk,jf->kf", weights[layer_no], grad_pre_norm, precision=HIGH)
        input_grad = lax.psum_scatter(input_terms, "neuron", scatter_dimension=0, tiled=True)
        grad_weight = lax.psum(weight_local, "batch")
        upstream = upstream + input_grad
        grad_parts[layer_no] = (grad_weight, grad_gain, grad_shift, grad_decay)
    grad_weights = jnp.stack([grad_parts[layer_no][0] for layer_no in range(LAYERS)])
    grad_gains = jnp.stack([grad_parts[layer_no][1] for layer_no in range(LAYERS)])
    grad_shifts = jnp.stack([grad_parts[layer_no][2] for layer_no in range(LAYERS)])
    grad_decays = jnp.stack([grad_parts[layer_no][3] for layer_no in range(LAYERS)])
    return (layer_in, upstream, grad_weights, grad_gains, grad_shifts, grad_decays, grad_shifts)


def solution(mesh):
    if (mesh.shape["batch"], mesh.shape["neuron"]) == (4, 8):
        cut = Mesh(mesh.devices.reshape(2, 2, 2, 2, 2), ("y", "x", "h", "l", "c"))
        batch, neuron, body = ("y", "x"), ("h", "l", "c"), half_features
    else:
        cut, batch, neuron, body = mesh, "batch", "neuron", split_features
    in_specs = (
        P(neuron, batch),
        P(None, neuron, None),
        P(None, neuron),
        P(None, neuron),
        P(None, neuron),
        P(None, neuron),
        P(batch),
        P(batch, None),
        P(neuron, batch),
    )
    out_specs = (
        P(neuron, batch),
        P(neuron, batch),
        P(None, neuron, None),
        P(None, neuron),
        P(None, neuron),
        P(None, neuron),
        P(None, neuron),
    )
    return jax.shard_map(
        body, mesh=cut, in_specs=in_specs, out_specs=out_specs, check_vma=False
    )
```

```python
from functools import partial
import math

import jax
import jax.numpy as jnp
from jax import lax
from jax.experimental import pallas as pl
from jax.experimental.pallas import tpu as pltpu
from jax.sharding import Mesh, PartitionSpec as P

LAYERS = 2
EPS = 1e-05
HIGH = lax.Precision.HIGHEST
ROOT_TWO = math.sqrt(2.0)
ROOT_TWO_PI = math.sqrt(2.0 * math.pi)
F32 = jnp.float32
BF16 = jnp.bfloat16
LANES = 128
VMEM_LIMIT = 24 * 1024 * 1024
SMEM_SPEC = pl.BlockSpec(memory_space=pltpu.SMEM)
VMEM_SPEC = pl.BlockSpec(memory_space=pltpu.VMEM)


FLIP2 = [(0, 1), (1, 0)]
DIAGONAL = [(0, 3), (1, 2), (2, 1), (3, 0)]


def swap_half(array):
    return lax.ppermute(array, "l", FLIP2)


def after(value, *others):
    return lax.optimization_barrier((value, others))[0]


def split(value):
    high = value.astype(BF16)
    return high, (value - high.astype(F32)).astype(BF16)


def dot(a, b, dims):
    return lax.dot_general(a, b, (dims, ((), ())), preferred_element_type=F32)


NT = ((1,), (1,))
NN = ((1,), (0,))


def in_hbm(array):
    return pltpu.with_memory_space_constraint(array, pltpu.HBM)


def call(body, out_shape, hbm_outs=(), **kwargs):
    if hbm_outs:
        out_shape = [
            pltpu.HBM(a.shape, a.dtype) if i in hbm_outs else a for i, a in enumerate(out_shape)
        ]
    return pl.pallas_call(
        body,
        out_shape=out_shape,
        compiler_params=pltpu.CompilerParams(vmem_limit_bytes=VMEM_LIMIT),
        **kwargs,
    )


def cost(flops, byte_count):
    return pl.CostEstimate(flops=int(flops) // 64, bytes_accessed=int(byte_count) // 64, transcendentals=0)


def pack_body(frames, place_ref, in_ref, near_ref, far_ref, turned):
    slots = in_ref.shape[1]
    for start in range(0, slots, LANES):
        turned[start : start + LANES, :] = in_ref[:, start : start + LANES].T
    for rel in range(4):
        first = pl.multiple_of(place_ref[rel] * frames, 8)
        out = (near_ref, far_ref)[rel // 2]
        out[(rel % 2) * frames : (rel % 2 + 1) * frames, :] = turned[pl.ds(first, frames), :]


def pack(place, array, frames, waits=False):
    width, slots = array.shape
    out = jax.ShapeDtypeStruct((2 * frames, width), F32)
    return call(
        partial(pack_body, frames),
        grid=(1,),
        out_shape=[out, out],
        in_specs=[SMEM_SPEC, pl.BlockSpec((width, slots), lambda i: (0, 0))],
        out_specs=[pl.BlockSpec(out.shape, lambda i: (0, 0))] * 2,
        scratch_shapes=[pltpu.VMEM((slots, width), F32)],
        hbm_outs=(0, 1) if waits else (),
        cost_estimate=cost(0, 8 * width * slots),
        name="pack",
    )(place, in_hbm(array))


def part_spec(part, frames):
    array, i = part
    if i is None:
        return pl.BlockSpec(array.shape, lambda *_: (0,) * array.ndim)
    return pl.BlockSpec((frames, array.shape[1]), lambda *_: (i, 0))


def arrays_of(parts):
    return [array for array, _ in parts]


def unpack_body(frames, place_ref, *refs):
    ins, out_ref, turned = refs[:4], refs[4], refs[5]
    slots = out_ref.shape[1]
    for rel in range(4):
        first = pl.multiple_of(place_ref[rel] * frames, 8)
        turned[pl.ds(first, frames), :] = ins[rel][...]
    for start in range(0, slots, LANES):
        out_ref[:, start : start + LANES] = turned[start : start + LANES, :].T


def unpack(place, parts, frames, waited=False):
    width = parts[0][0].shape[1]
    slots = 4 * frames
    return call(
        partial(unpack_body, frames),
        grid=(1,),
        out_shape=jax.ShapeDtypeStruct((width, slots), F32),
        in_specs=[SMEM_SPEC] + [part_spec(part, frames) for part in parts],
        out_specs=pl.BlockSpec((width, slots), lambda i: (0, 0)),
        scratch_shapes=[pltpu.VMEM((slots, width), F32)],
        cost_estimate=cost(0, 8 * width * slots),
        name="unpack",
    )(place, *[in_hbm(a) if waited else a for a in arrays_of(parts)])


def merge_body(kept_ref, come_ref, out_ref):
    frames, columns = kept_ref.shape
    width = columns // 2
    for i in range(2):
        some = slice(i * width, (i + 1) * width)
        out_ref[i * frames : (i + 1) * frames, :] = kept_ref[:, some] + come_ref[:, some]


def merge(kept, half, come):
    frames, columns = come.shape
    return call(
        merge_body,
        grid=(1,),
        out_shape=jax.ShapeDtypeStruct((2 * frames, columns // 2), F32),
        in_specs=[
            pl.BlockSpec((frames, columns), lambda i: (0, half)),
            pl.BlockSpec((frames, columns), lambda i: (0, 0)),
        ],
        out_specs=pl.BlockSpec((2 * frames, columns // 2), lambda i: (0, 0)),
        cost_estimate=cost(0, 12 * frames * columns),
        name="merge",
    )(kept, come)


def project_body(n_parts, n_flat, spots, n_weights, first, with_acc, with_stats, with_params, cols_ref, place_ref, *refs):
    del cols_ref

    def take(n):
        nonlocal refs
        some, refs = refs[:n], refs[n:]
        return some

    parts, flat_parts, weights = take(n_parts), take(n_flat), take(n_weights)
    acc, valid, stats_in, params = take(with_acc), take(with_stats > 0), take(with_stats > 1), take(with_params)
    (out_ref,) = take(1)
    stats, flat = take(with_stats > 0), take(n_flat > 0)
    x_high, x_low, far_ref = refs
    step = pl.program_id(0)
    width = x_high.shape[2]

    @pl.when(step == 0)
    def _():
        for block, part in zip(spots, parts):
            for start in range(0, part.shape[1], width):
                high, low = split(part[:, start : start + width])
                x_high[block + start // width] = high
                x_low[block + start // width] = low
        column = 0
        for part in flat_parts:
            flat[0][:, column : column + part.shape[1]] = part[...]
            column += part.shape[1]
        if with_acc:
            out_ref[...] = acc[0][...]
        else:
            out_ref[...] = jnp.zeros_like(out_ref)

    stacked = jnp.concatenate([x_high[step], x_low[step], x_high[step]], axis=1)
    for block, weight in enumerate(weight_blocks(place_ref, weights, far_ref)):
        w_high, w_low = split(weight)
        columns = slice(block * width, (block + 1) * width)
        out_ref[:, columns] += dot(stacked, jnp.concatenate([w_high, w_high, w_low], axis=1), NT)

    if with_stats:
        (stats_ref,) = stats

        @pl.when(step == pl.num_programs(0) - 1)
        def _():
            if stats_in:
                stats_ref[...] = stats_in[0][...]
            own = jnp.sum(valid[0][...], axis=0, keepdims=True)
            per = width // LANES
            for row in range(out_ref.shape[1] // LANES):
                z = out_ref[:, row * LANES : (row + 1) * LANES]
                total = jnp.sum(valid[0][...] * z, axis=0, keepdims=True)
                centred = valid[0][...] * (z - total / own)
                squares = jnp.sum(centred * centred, axis=0, keepdims=True)
                at = place_ref[first + row // per] * per + row % per
                stats_ref[0, pl.ds(at, 1), :] = total
                stats_ref[1, pl.ds(at, 1), :] = squares
                stats_ref[2, pl.ds(at, 1), :] = own
            if with_params:
                rest = params[0].shape[0] - 8
                stats_ref[3] = params[0][:8, :]
                stats_ref[4] = jnp.zeros_like(stats_ref[4])
                stats_ref[4, :rest, :] = params[0][8:, :]


def weight_specs(weights, layer, pairs=2):
    specs = []
    for weight in weights:
        if weight.ndim == 3:
            shape = (1, weight.shape[1], pairs * weight.shape[1])
            specs.append(pl.BlockSpec(shape, lambda s, cols, *_: (layer, 0, cols[s])))
        else:
            shape = (weight.shape[0], pairs * 4 * weight.shape[0])
            specs.append(pl.BlockSpec(shape, lambda s, cols, *_: (0, cols[s])))
    return specs


def far_scratch(width, pairs=2):
    return pltpu.VMEM((2, width, pairs * width), F32)


def weight_blocks(place_ref, refs, far_ref):
    near = [ref[0] for ref in refs if len(ref.shape) == 3]
    pieces = [ref for ref in refs if len(ref.shape) == 2]
    far = []
    for i in range(len(pieces) // 4):
        for rel, piece in enumerate(pieces[4 * i : 4 * i + 4]):
            rows = piece.shape[0]
            row = 2 * (place_ref[4] ^ (rel // 2)) + (place_ref[5] ^ (rel % 2))
            far_ref[i, pl.ds(pl.multiple_of(row * rows, rows), rows), :] = piece[...]
        far.append(far_ref[i])
    return near + far


def project(
    place, frames, parts, blocks, weights, layer, acc=None, valid=None, stats=None, params=None, flat=()
):
    near = weights[0].ndim == 3
    units = sum(1 if w.ndim == 3 else 0.25 for w in weights)
    width = weights[0].shape[1] if near else 4 * weights[0].shape[0]
    n = blocks.shape[0]
    spots, block = [], 0
    for array, _ in parts:
        spots.append(block)
        block += array.shape[1] // width
    full = pl.BlockSpec(memory_space=pltpu.VMEM)
    in_specs = [part_spec(part, frames) for part in (*parts, *flat)]
    in_specs += weight_specs(weights, layer, 1)
    operands = arrays_of(parts) + arrays_of(flat) + [in_hbm(w) for w in weights]
    array = jax.ShapeDtypeStruct((frames, int(units) * width), F32)
    array_spec = pl.BlockSpec(array.shape, lambda s, cols, place: (0, 0))
    out_shape, out_specs = [array], [array_spec]
    if acc is not None:
        in_specs.append(array_spec)
        operands.append(in_hbm(acc))
    if valid is not None:
        in_specs.append(full)
        operands.append(valid)
        shape = (3 if params is None else 5, 4 * width // LANES, LANES)
        out_shape.append(jax.ShapeDtypeStruct(shape, F32))
        out_specs.append(pl.BlockSpec(shape, lambda s, cols, place: (0, 0, 0)))
    for extra in (stats, params):
        if extra is not None:
            in_specs.append(full)
            operands.append(extra)
    if flat:
        out_shape.append(jax.ShapeDtypeStruct((frames, 4 * width), F32))
        out_specs.append(pl.BlockSpec((frames, 4 * width), lambda s, cols, place: (0, 0)))
    return call(
        partial(
            project_body,
            len(parts),
            len(flat),
            spots,
            len(weights),
            0 if near else 2,
            acc is not None,
            (valid is not None) + (stats is not None),
            params is not None,
        ),
        grid_spec=pltpu.PrefetchScalarGridSpec(
            num_scalar_prefetch=2,
            grid=(n,),
            in_specs=in_specs,
            out_specs=out_specs,
            scratch_shapes=[pltpu.VMEM((n, frames, width), BF16)] * 2 + [far_scratch(width, 1)],
        ),
        out_shape=out_shape,
        hbm_outs=(0, len(out_shape) - 1) if flat else (0,),
        cost_estimate=cost(6 * frames * n * width * units * width, 4 * n * width * units * width),
        name="project",
    )(blocks, place, *operands)


def to_relative(place_ref, spread, rows_ref, value, slot):
    per = value.shape[0] // 4
    spread[...] = value
    for rel in range(4):
        first = place_ref[rel] * per
        for row in range(per):
            rows_ref[slot, rel * per + row : rel * per + row + 1, :] = spread[
                pl.ds(first + row, 1), :
            ]


def tree(values):
    while len(values) > 1:
        values = [a + b for a, b in zip(values[::2], values[1::2])]
    return values[0]


def gathered(ref, slot):
    return [ref[i] for i in range(slot, ref.shape[0], ref.shape[0] // 16)]


def norm_terms(stats_ref):
    each = [gathered(stats_ref, slot) for slot in range(3)]
    totals, squares, owns = each
    count = tree(owns)
    mean = tree(totals) / count
    away = [total / own - mean for total, own in zip(totals, owns)]
    spread = tree([s + n * a * a for s, n, a in zip(squares, owns, away)])
    return count, mean, lax.rsqrt(spread / count + EPS)


CHUNKS = 4


def columns_of(refs, row):
    for ref in refs:
        if row * LANES < ref.shape[1]:
            return ref[:, row * LANES : (row + 1) * LANES]
        row -= ref.shape[1] // LANES


def recur_body(n_z, last, layer, spread_params, place_ref, gate_ref, *refs):
    z_refs, refs = refs[:n_z], refs[n_z:]
    (stats_ref, params_ref, valid_ref, x_ref), refs = refs[:4], refs[4:]
    outs, refs = refs[: 1 + 3 * last], refs[1 + 3 * last :]
    if spread_params:
        state_ref, slope_ref, params_out, rows, spread, held, drive_s, state_s, slope_s = refs
    else:
        state_ref, slope_ref, rows, spread, held, drive_s, state_s, slope_s = refs
    frames, features = x_ref.shape
    blocks = features // LANES
    per = blocks // 4
    chunk = pl.program_id(0)

    @pl.when(chunk == 0)
    def _():
        if spread_params:
            for rel in range(4):
                first = place_ref[rel] * (stats_ref.shape[0] // 16) + 3
                for row in range(LAYERS * 3 * per):
                    at = rel * per + row % per
                    params_out[row // per, at : at + 1, :] = stats_ref[
                        first + row // 8, row % 8 : row % 8 + 1, :
                    ]
            params = [params_out[3 * layer + i] for i in range(3)]
        else:
            params = [params_ref[3 * layer + i] for i in range(3)]
        _, mean, inv_std = norm_terms(stats_ref)
        to_relative(place_ref, spread, rows, mean, 0)
        to_relative(place_ref, spread, rows, inv_std, 1)
        rows[1] = rows[1] * params[0]
        rows[2] = params[1]
        rows[3] = params[2]
        held[...] = jnp.zeros_like(held)

    for row in range(blocks):
        drive_s[row * frames : (row + 1) * frames, :] = (
            columns_of(z_refs, row) - rows[0, row : row + 1, :]
        ) * rows[1, row : row + 1, :] + rows[2, row : row + 1, :]
    decay = rows[3]

    def step(t, state):
        at = pl.ds(t, blocks, stride=frames)
        pre = drive_s[at, :] + decay * state
        half = 0.5 + 0.5 * lax.erf(pre * (1.0 / ROOT_TWO))
        gate = gate_ref[chunk * frames + t] > 0.0
        slope = half + pre * jnp.exp(-0.5 * pre * pre) * (1.0 / ROOT_TWO_PI)
        state = jnp.where(gate, pre * half, state)
        state_s[at, :] = state
        slope_s[at, :] = jnp.where(gate, slope, 0.0)
        return state

    held[...] = lax.fori_loop(0, frames, step, held[...], unroll=8)
    valid = valid_ref[...]
    for row in range(blocks):
        lanes = slice(row * LANES, (row + 1) * LANES)
        state = state_s[row * frames : (row + 1) * frames, :]
        state_ref[:, lanes] = state
        slope_ref[:, lanes] = slope_s[row * frames : (row + 1) * frames, :]
        value = x_ref[:, lanes] + valid * state
        out, at = (outs[row // per], row % per) if last else (outs[0], row)
        out[:, at * LANES : (at + 1) * LANES] = value


def recur(layer, place, gate, z, stats, params, valid, x, last):
    frames, features = x.shape
    blocks = features // LANES
    some = frames // CHUNKS
    whole = lambda array: pl.BlockSpec(array.shape, lambda i: (0,) * array.ndim)
    by_chunk = lambda array: pl.BlockSpec((some, array.shape[1]), lambda i: (i, 0))
    full = jax.ShapeDtypeStruct((frames, features), F32)
    piece = jax.ShapeDtypeStruct((frames, features // 4), F32)
    out_shape = [piece] * 4 if last else [full]
    out_shape += [full, full]
    out_specs = [by_chunk(a) for a in out_shape]
    spread_params = params is None
    if spread_params:
        out_shape.append(jax.ShapeDtypeStruct((3 * LAYERS, blocks, LANES), F32))
        out_specs.append(whole(out_shape[-1]))
        params = valid
    return call(
        partial(recur_body, len(z), last, layer, spread_params),
        grid=(CHUNKS,),
        in_specs=[SMEM_SPEC, SMEM_SPEC]
        + [by_chunk(a) for a in z]
        + [whole(a) for a in (stats, params)]
        + [by_chunk(a) for a in (valid, x)],
        out_specs=out_specs,
        out_shape=out_shape,
        hbm_outs=tuple(range(len(out_shape) - spread_params)) if last else (1, 2),
        scratch_shapes=[
            pltpu.VMEM((4, blocks, LANES), F32),
            pltpu.VMEM((blocks, LANES), F32),
            pltpu.VMEM((blocks, LANES), F32),
        ]
        + [pltpu.VMEM((blocks * some, LANES), F32)] * 3,
        cost_estimate=cost(100 * frames * features, 20 * frames * features),
        name="recur",
    )(place, gate, *[in_hbm(a) for a in z], stats, params, valid, in_hbm(x))


def back_body(n_z, n_ups, spots, layer, place_ref, gate_ref, *refs):
    z_refs, refs = refs[:n_z], refs[n_z:]
    (stats_ref, params_ref), refs = refs[:2], refs[2:]
    ups, (state_ref, slope_ref), refs = refs[:n_ups], refs[n_ups : n_ups + 2], refs[n_ups + 2 :]
    grad_ref, sums_ref, rows, spread, held, up_s, state_s, slope_s = refs
    frames, features = state_ref.shape
    blocks = features // LANES
    per = blocks // 4
    tall = frames + 8
    step_no = pl.program_id(0)
    chunk = pl.num_programs(0) - 1 - step_no

    @pl.when(step_no == 0)
    def _():
        _, mean, inv_std = norm_terms(stats_ref)
        to_relative(place_ref, spread, rows, mean, 0)
        to_relative(place_ref, spread, rows, inv_std, 1)
        held[...] = jnp.zeros_like(held)

    for row in range(blocks):
        lanes = slice(row * LANES, (row + 1) * LANES)
        base = row * frames
        up = None
        for (_, column), part in zip(spots, ups):
            if column <= row * LANES < column + part.shape[1]:
                value = part[:, row * LANES - column : (row + 1) * LANES - column]
                up = value if up is None else up + value
        up_s[base : base + frames, :] = up
        state_s[row * tall : row * tall + 8, :] = jnp.zeros((8, LANES), F32)
        state_s[row * tall + 8 : (row + 1) * tall, :] = state_ref[:, lanes]
        slope_s[base : base + frames, :] = slope_ref[:, lanes]
    decay = params_ref[3 * layer + 2]

    def step(i, carry):
        t = frames - 1 - i
        at = pl.ds(t, blocks, stride=frames)
        slope = slope_s[at, :]
        gate = gate_ref[chunk * frames + t]
        total = gate * up_s[at, :] + carry
        up_s[at, :] = total * slope
        return total * (slope * decay + (1.0 - gate))

    held[0] = lax.fori_loop(0, frames, step, held[0], unroll=8)
    held[4] += held[1] * state_s[pl.ds(tall - 1, blocks, stride=tall), :]
    held[1] = up_s[pl.ds(0, blocks, stride=frames), :]
    for row in range(blocks):
        lanes = slice(row * LANES, (row + 1) * LANES)
        grad = up_s[row * frames : (row + 1) * frames, :]
        grad_ref[:, lanes] = grad
        zhat = (columns_of(z_refs, row) - rows[0, row : row + 1, :]) * rows[1, row : row + 1, :]
        before = state_s[row * tall + 7 : row * tall + 7 + frames, :]
        for slot, value in enumerate((grad * zhat, grad, grad * before)):
            held[2 + slot, row : row + 1, :] += jnp.sum(value, axis=0, keepdims=True)

    @pl.when(chunk == 0)
    def _():
        for row in range(blocks):
            at = place_ref[row // per] * per + row % per
            for slot in range(3):
                sums_ref[slot, pl.ds(at, 1), :] = held[2 + slot, row : row + 1, :]


def spots_of_sum(parts, width):
    spots, column = [], 0
    for array, _ in parts:
        spots.append((0, column % (4 * width)))
        column += array.shape[1]
    return spots


def back(layer, place, gate, z, stats, params, ups, states, slopes):
    frames, features = states.shape
    width = features // 4
    blocks = features // LANES
    some = frames // CHUNKS
    whole = lambda array: pl.BlockSpec(array.shape, lambda i: (0,) * array.ndim)

    def by_chunk(array, first=0):
        return pl.BlockSpec(
            (some, array.shape[1]), lambda i: ((first or 0) * CHUNKS + CHUNKS - 1 - i, 0)
        )

    out_shape = [
        jax.ShapeDtypeStruct((frames, features), F32),
        jax.ShapeDtypeStruct((3, blocks, LANES), F32),
    ]
    return call(
        partial(back_body, len(z), len(ups), spots_of_sum(ups, width), layer),
        grid=(CHUNKS,),
        in_specs=[SMEM_SPEC] * 2
        + [by_chunk(a) for a in z]
        + [whole(a) for a in (stats, params)]
        + [by_chunk(*up) for up in ups]
        + [by_chunk(a) for a in (states, slopes)],
        out_specs=[by_chunk(out_shape[0]), whole(out_shape[1])],
        out_shape=out_shape,
        scratch_shapes=[
            pltpu.VMEM((2, blocks, LANES), F32),
            pltpu.VMEM((blocks, LANES), F32),
            pltpu.VMEM((5, blocks, LANES), F32),
            pltpu.VMEM((blocks * some, LANES), F32),
            pltpu.VMEM((blocks * (some + 8), LANES), F32),
            pltpu.VMEM((blocks * some, LANES), F32),
        ],
        cost_estimate=cost(30 * frames * features, 20 * frames * features),
        name="back",
    )(
        place,
        gate,
        *[in_hbm(a) for a in z],
        stats,
        params,
        *arrays_of(ups),
        in_hbm(states),
        in_hbm(slopes),
    )


def input_terms(high_s, low_s, weights):
    left, right = [], []
    for block, weight in enumerate(weights):
        w_high, w_low = split(weight)
        left += [high_s[block], low_s[block], high_s[block]]
        right += [w_high, w_high, w_low]
    return dot(jnp.concatenate(left, axis=1), jnp.concatenate(right, axis=0), NN)


def norm_back_body(n_z, split_terms, layer, cols_ref, place_ref, grad_ref, *refs):
    del cols_ref
    z_refs, refs = refs[:n_z], refs[n_z:]
    params_ref, valid_ref, stats_ref, sums_ref, *refs = refs
    weights, refs = refs[:10], refs[10:]
    if split_terms:
        out_ref, leave_ref, near_term_ref, far_term_ref, sums_out_ref, *refs = refs
        term_refs, starts = (far_term_ref, near_term_ref), (0, 0)
    else:
        out_ref, leave_ref, term_ref, sums_out_ref, *refs = refs
        term_refs, starts = (term_ref, term_ref), (2 * grad_ref.shape[1] // 4, 0)
    rows, spread, high_s, low_s, far_ref = refs
    blocks = grad_ref.shape[1] // LANES
    width = high_s.shape[2]
    per = width // LANES

    @pl.when(pl.program_id(0) == 0)
    def _():
        count, mean, inv_std = norm_terms(stats_ref)
        to_relative(place_ref, spread, rows, mean, 0)
        to_relative(place_ref, spread, rows, inv_std, 1)
        rows[2] = rows[1] * params_ref[3 * layer]
        sums = [tree(gathered(sums_ref, slot)) for slot in range(3)]
        for slot in range(3):
            sums_out_ref[slot] = sums[slot]
        to_relative(place_ref, spread, rows, sums[0] / count, 3)
        to_relative(place_ref, spread, rows, sums[1] / count, 4)
        valid = valid_ref[...]
        for row in range(blocks):
            lanes = slice(row * LANES, (row + 1) * LANES)
            one = lambda slot: rows[slot, row : row + 1, :]
            zhat = (columns_of(z_refs, row) - one(0)) * one(1)
            value = one(2) * (grad_ref[:, lanes] - valid * (one(4) + zhat * one(3)))
            out_ref[:, lanes] = value
            if (row // per) % 2:
                at = (row // per // 2) * width + (row % per) * LANES
                leave_ref[:, at : at + LANES] = value
            high, low = split(value)
            inner = slice((row % per) * LANES, (row % per + 1) * LANES)
            high_s[row // per, :, inner] = high
            low_s[row // per, :, inner] = low

    value = input_terms(high_s, low_s, weight_blocks(place_ref, weights, far_ref))
    for step, (term_ref, first) in enumerate(zip(term_refs, starts)):

        @pl.when(pl.program_id(0) == step)
        def _():
            for pair in range(2):
                at = pl.multiple_of(((place_ref[0] & 1) ^ pair) * width, width)
                term_ref[:, pl.ds(first + at, width)] = value[
                    :, pair * width : (pair + 1) * width
                ]


def norm_back(columns, place, grad, z, params, valid, stats, sums, weights, layer, split_terms):
    frames, features = grad.shape
    width = features // 4
    blocks = features // LANES
    whole = lambda array: pl.BlockSpec(array.shape, lambda s, cols, place: (0,) * array.ndim)
    operands = [grad, *[in_hbm(a) for a in z], params, valid, stats, sums]
    full = jax.ShapeDtypeStruct((frames, features), F32)
    half = jax.ShapeDtypeStruct((frames, 2 * width), F32)
    terms = [half, half] if split_terms else [full]
    out_shape = [full, half, *terms, jax.ShapeDtypeStruct((3, blocks, LANES), F32)]
    return call(
        partial(norm_back_body, len(z), split_terms, layer),
        grid_spec=pltpu.PrefetchScalarGridSpec(
            num_scalar_prefetch=2,
            grid=(2,),
            in_specs=[whole(a) for a in operands] + weight_specs(weights, layer),
            out_specs=[whole(a) for a in out_shape],
            scratch_shapes=[
                pltpu.VMEM((5, blocks, LANES), F32),
                pltpu.VMEM((blocks, LANES), F32),
                pltpu.VMEM((4, frames, width), BF16),
                pltpu.VMEM((4, frames, width), BF16),
                far_scratch(width),
            ],
        ),
        out_shape=out_shape,
        hbm_outs=(0,),
        cost_estimate=cost(6 * frames * features * features, 4 * features * features),
        name="norm_back",
    )(columns, place, *operands, *[in_hbm(w) for w in weights])


def own_terms_body(n_ups, spots, cols_ref, place_ref, grad_ref, *refs):
    del cols_ref
    ups, refs = refs[:n_ups], refs[n_ups:]
    weights, refs = refs[:10], refs[10:]
    out_ref, high_s, low_s, far_ref = refs
    width = high_s.shape[2]
    step = pl.program_id(0)

    @pl.when(step == 0)
    def _():
        for block in range(4):
            high, low = split(grad_ref[:, block * width : (block + 1) * width])
            high_s[block] = high
            low_s[block] = low

    value = input_terms(high_s, low_s, weight_blocks(place_ref, weights, far_ref))
    for pair in range(2):
        at = pl.multiple_of(((place_ref[0] & 1) ^ pair) * width, width)
        out_ref[:, pl.ds(at, width)] = value[:, pair * width : (pair + 1) * width]
    for half in range(2):

        @pl.when(step == half)
        def _():
            first = 2 * half * width
            for (_, column), up in zip(spots, ups):
                low = max(column, first)
                high = min(column + up.shape[1], first + 2 * width)
                if low < high:
                    out_ref[:, low - first : high - first] += up[:, low - column : high - column]


def own_terms(columns, place, grad, ups, weights, layer):
    frames, features = grad.shape
    width = features // 4
    whole = lambda array: pl.BlockSpec(array.shape, lambda s, cols, place: (0,) * array.ndim)
    step_block = pl.BlockSpec((frames, 2 * width), lambda s, cols, place: (0, s))
    return call(
        partial(own_terms_body, len(ups), spots_of_sum(ups, width)),
        grid_spec=pltpu.PrefetchScalarGridSpec(
            num_scalar_prefetch=2,
            grid=(2,),
            in_specs=[whole(grad)]
            + [part_spec(up, frames) for up in ups]
            + weight_specs(weights, layer),
            out_specs=step_block,
            scratch_shapes=[pltpu.VMEM((4, frames, width), BF16)] * 2 + [far_scratch(width)],
        ),
        out_shape=jax.ShapeDtypeStruct((frames, features), F32),
        cost_estimate=cost(6 * frames * features * features, 4 * features * features),
        name="own_terms",
    )(columns, place, in_hbm(grad), *arrays_of(ups), *[in_hbm(w) for w in weights])


def prepare_body(lists_ref, place_ref, own_ref, near_ref, high_ref, low_ref):
    del lists_ref
    padded = high_ref.shape[0] // 2
    width = high_ref.shape[1] // 2
    for clip, part in enumerate((own_ref, near_ref)):
        rows = part.shape[0]
        for dc in range(2):
            at = pl.multiple_of((place_ref[6] ^ clip ^ dc) * width, width)
            high, low = split(part[:, dc * width : (dc + 1) * width])
            high_ref[clip * padded : clip * padded + rows, pl.ds(at, width)] = high
            low_ref[clip * padded : clip * padded + rows, pl.ds(at, width)] = low
        zeros = jnp.zeros((padded - rows, 2 * width), BF16)
        high_ref[clip * padded + rows : (clip + 1) * padded, :] = zeros
        low_ref[clip * padded + rows : (clip + 1) * padded, :] = zeros


def prepare(place, own, near):
    frames, features = own.shape
    width = features // 4
    padded = -(-frames // LANES) * LANES
    in_spec = pl.BlockSpec((frames, 2 * width), lambda s, *_: (0, s))
    out = jax.ShapeDtypeStruct((2 * padded, features), BF16)
    out_spec = pl.BlockSpec((2 * padded, 2 * width), lambda s, order, place: (0, order[s]))
    order = jnp.stack([place[0] >> 1, 1 - (place[0] >> 1)])
    return call(
        prepare_body,
        grid_spec=pltpu.PrefetchScalarGridSpec(
            num_scalar_prefetch=2,
            grid=(2,),
            in_specs=[in_spec, in_spec],
            out_specs=[out_spec, out_spec],
        ),
        out_shape=[out, out],
        hbm_outs=(0, 1),
        cost_estimate=cost(0, 16 * frames * features),
        name="prepare",
    )(order, place, in_hbm(own), in_hbm(near))


def product(g_high, g_low, x_high, x_low):
    return dot(g_high, x_high, NN) + (dot(g_high, x_low, NN) + dot(g_low, x_high, NN))


def weight_body(turn, place_ref, *refs):
    if turn:
        grad_ref, near_ref, x_high, x_low, kept, sent, g_high, g_low, t_high, t_low = refs

        @pl.when(pl.program_id(0) == 0)
        def _():
            frames, features = grad_ref.shape
            width = features // 4
            rows = width // 4
            padded = t_high.shape[1] // 2
            t_high[...] = jnp.zeros_like(t_high)
            t_low[...] = jnp.zeros_like(t_low)
            for clip in range(2):
                for dh in range(2):
                    if clip == 0:
                        part = grad_ref[:, 2 * dh * width : (2 * dh + 1) * width]
                    else:
                        part = near_ref[:, dh * width : (dh + 1) * width]
                    high, low = split(part.T)
                    at = (
                        slice(dh * width, (dh + 1) * width),
                        slice(clip * padded, clip * padded + frames),
                    )
                    t_high[at] = high
                    t_low[at] = low
            for group in range(8):
                first, second, dh = group // 4, group // 2 % 2, group % 2
                core = place_ref[6]
                y = place_ref[4] ^ (first * core + second * (1 - core))
                x = place_ref[5] ^ (first * (1 - core) + second * core)
                at = pl.multiple_of(dh * width + (2 * y + x) * rows, rows)
                g_high[group * rows : (group + 1) * rows, :] = t_high[pl.ds(at, rows), :]
                g_low[group * rows : (group + 1) * rows, :] = t_low[pl.ds(at, rows), :]

    else:
        g_high, g_low, x_high, x_low, kept, sent = refs
    half = g_high.shape[0] // 2
    value = product(g_high[...], g_low[...], x_high[...], x_low[...])
    kept[...] = value[:half].reshape(kept.shape)
    sent[...] = value[half:].reshape(sent.shape)


def weight_rows(side, place, grads, x_split, width):
    turn = side == 0
    whole = lambda array: pl.BlockSpec(array.shape, lambda s, place: (0,) * array.ndim)
    x_spec = pl.BlockSpec((x_split[0].shape[0], width), lambda s, place: (0, s))
    shape = (2, 2, width // 4, 4 * width)
    out_shape = [jax.ShapeDtypeStruct(shape, F32)] * 2
    out_specs = [pl.BlockSpec(shape[:3] + (width,), lambda s, place: (0, 0, 0, s))] * 2
    scratch = []
    if turn:
        turned = (2 * width, x_split[0].shape[0])
        out_shape += [jax.ShapeDtypeStruct(turned, BF16)] * 2
        out_specs += [whole(out_shape[-1])] * 2
        scratch = [pltpu.VMEM(turned, BF16)] * 2
    return call(
        partial(weight_body, turn),
        grid_spec=pltpu.PrefetchScalarGridSpec(
            num_scalar_prefetch=1,
            grid=(4,),
            in_specs=[whole(a) for a in grads] + [x_spec] * 2,
            out_specs=out_specs,
            scratch_shapes=scratch,
        ),
        out_shape=out_shape,
        hbm_outs=(0,),
        cost_estimate=cost(12 * x_split[0].shape[0] * width * 4 * width, 4 * 8 * width * width),
        name="weight_rows",
    )(place, *([in_hbm(grads[0]), grads[1]] if turn else grads), *[in_hbm(x) for x in x_split])


def step_body(n, widths, cut, *refs):
    ins, outs = refs[: 2 * n], refs[2 * n :]
    starts = [sum(widths[:i]) for i in range(len(widths))]
    column = 0
    for i in range(n):
        total = ins[2 * i][...] + ins[2 * i + 1][...]
        end = column + total.shape[-1]
        for j, (start, columns) in enumerate(zip(starts, widths)):
            low, high = max(start, column), min(start + columns, end)
            if low < high:
                to = (Ellipsis, slice(low - start, high - start))
                piece = total[..., low - column : high - column]
                if cut:
                    outs[2 * j][to] = piece[0]
                    outs[2 * j + 1][to] = piece[1]
                else:
                    outs[j][to] = piece
        column = end


def step_of(*pairs, cut=True, widths=None):
    shape = list(pairs[0][0].shape)
    widths = widths or [sum(pair[0].shape[-1] for pair in pairs)]
    outs = []
    for columns in widths:
        shape[-1] = columns
        out = jax.ShapeDtypeStruct(tuple(shape[1:] if cut else shape), F32)
        outs += [out] * (1 + cut)
    whole = lambda array: pl.BlockSpec(array.shape, lambda i: (0,) * array.ndim)
    operands = [array for pair in pairs for array in pair]
    return call(
        partial(step_body, len(pairs), widths, cut),
        grid=(1,),
        in_specs=[whole(a) for a in operands],
        out_specs=[whole(a) for a in outs],
        out_shape=outs,
        cost_estimate=cost(0, 4 * sum(a.size for a in operands)),
        name="reduction_step",
    )(*operands)


def plane_swap(array, step):
    pairs = []
    for i in range(8):
        over_x = (i % 2 == 0) == (step == 0)
        pairs.append((i, i ^ 2 if over_x else i ^ 4))
    return lax.ppermute(array, ("y", "x", "c"), pairs)


def plane_gather(share, *before):
    first = plane_swap(share, 0)
    second = plane_swap(share, 1)
    return [share, second, first, plane_swap(after(first, *before), 1)]


def assemble_body(place_ref, *refs):
    out_ref = refs[-1]
    core = place_ref[6]
    rows, columns = refs[0].shape
    quarter = columns // 4
    for i in range(4):
        first, second = i // 2, i % 2
        y = place_ref[4] ^ (first * core + second * (1 - core))
        x = place_ref[5] ^ (first * (1 - core) + second * core)
        at = pl.multiple_of((2 * y + x) * rows, rows)
        for side in range(2):
            for h in range(2):
                to = pl.multiple_of((2 * h + (place_ref[7] ^ side)) * quarter, quarter)
                some = slice((2 * side + h) * quarter, (2 * side + h + 1) * quarter)
                out_ref[0, pl.ds(at, rows), pl.ds(to, quarter)] = refs[i][:, some]


def assemble(place, pieces, layer, onto=None):
    rows, columns = 4 * pieces[0].shape[0], pieces[0].shape[1]
    aliases, extra, extra_specs = {}, [], []
    if onto is not None:
        aliases, extra = {1 + len(pieces): 0}, [onto]
        extra_specs = [pl.BlockSpec(memory_space=pl.ANY)]
    (out,) = call(
        assemble_body,
        grid=(1,),
        out_shape=[jax.ShapeDtypeStruct((LAYERS, rows, columns), F32)],
        hbm_outs=(0,),
        in_specs=[SMEM_SPEC]
        + [pl.BlockSpec(p.shape, lambda i: (0, 0)) for p in pieces]
        + extra_specs,
        out_specs=[pl.BlockSpec((1, rows, columns), lambda i: (layer, 0, 0))],
        input_output_aliases=aliases,
        cost_estimate=cost(0, 8 * rows * columns),
        name="assemble",
    )(place, *[p if extra else in_hbm(p) for p in pieces], *extra)
    return out


def half_features(inputs, weights, gains, shifts, decays, biases, lengths, frame_mask, grad_out):
    width, slots = inputs.shape
    clips, frames = frame_mask.shape
    depth = weights.shape[2]
    blocks = 4 * width // LANES
    y, x, h, l, c = (lax.axis_index(name) for name in ("y", "x", "h", "l", "c"))
    b = 2 * y + x
    numbers = [2 * (h ^ (rel // 2)) + (c ^ (rel % 2)) for rel in range(4)] + [y, x, c, l]
    place = jnp.stack(numbers).astype(jnp.int32)
    own_blocks, other_blocks = (
        jnp.stack(
            [2 * (2 * (h ^ (rel // 2)) + half) + (c ^ (rel % 2)) for rel in range(4)]
        ).astype(jnp.int32)
        for half in (l, 1 - l)
    )
    own_columns = jnp.stack([2 * h + l, 2 * (1 - h) + l]).astype(jnp.int32)
    other_columns = jnp.stack([2 * (1 - h) + 1 - l, 2 * h + 1 - l]).astype(jnp.int32)
    rows = width // 4

    clip = 2 * h + c
    seen = lax.dynamic_index_in_dim(frame_mask, clip, 0, keepdims=False)
    length = lax.dynamic_index_in_dim(lengths, clip, 0, keepdims=False)
    moments = jnp.arange(frames, dtype=jnp.int32)
    gate = ((moments < length) & ((seen == 1) | (moments == 0))).astype(F32)
    valid = jnp.broadcast_to(gate[:, None], (frames, LANES))

    def far_share(layer):
        return lax.dynamic_slice(weights, (layer, b * rows, 0), (1, rows, depth))[0]

    def over_h(array):
        return lax.ppermute(array, "h", FLIP2)

    def over_c(array):
        return lax.ppermute(array, "c", FLIP2)

    def over_second(array):
        return plane_swap(array, 1)

    def four_of(near_rows, far_rows):
        return [
            (near_rows, 0),
            (over_c(near_rows), 1),
            (far_rows, 0),
            (over_c(far_rows), 1),
        ]

    def far_pieces(share):
        both = lax.ppermute(share, ("y", "x"), DIAGONAL)
        return [share, lax.ppermute(share, "x", FLIP2), lax.ppermute(share, "y", FLIP2), both]

    near = over_c(weights)
    share = far_share(0)
    close, away = pack(place, after(inputs, share), frames)
    share = over_h(share)
    away = over_h(away)
    other_close = swap_half(close)
    up_close, up_away = pack(place, after(grad_out, close), frames, waits=True)
    share = after(share, up_close, valid, near, other_close)
    pieces = far_pieces(share)
    away = after(away, pieces[1:])
    half_weights = [[weights, near, *pieces, *map(over_c, after(pieces, away))]]
    own = four_of(after(close, away), away)
    other_away = swap_half(away)
    others = [(other_close, 0), (over_c(other_close), 1)]
    params = jnp.stack([gains, shifts + biases, decays], axis=1)
    own_params = params.reshape(LAYERS * 3 * width // LANES, LANES)
    params = None

    def gather(array, axes):
        return lax.all_gather(array, axes, tiled=True)

    weight = half_weights[0]
    early = jnp.concatenate([own_blocks, other_blocks[:2]])
    z, own_flat = project(place, frames, own + others, early, weight, 0, flat=own)
    others += [(other_away, 0), (over_c(after(other_away, z)), 1)]
    z, stats, other_flat = project(
        place,
        frames,
        others[2:],
        other_blocks[2:],
        weight,
        0,
        z,
        valid,
        params=own_params,
        flat=others,
    )
    z = [z]
    stats = gather(stats, ("h", "c"))
    share = over_c(lax.ppermute(after(far_share(1), stats), ("h", "c"), DIAGONAL))
    stats = gather(stats, ("y", "x"))
    x, states, slopes, params = recur(0, place, gate, z, stats, None, valid, own_flat, False)
    own_near, other_near = over_c(after(own_flat, z[0])), over_c(after(other_flat, z[0]))
    x_near = over_c(x)
    own_split = prepare(place, after(own_flat, x_near), own_near)
    other_split = prepare(place, after(other_flat, x_near), other_near)
    saved = [(own_split, other_split, z, stats, states, slopes)]

    pieces = far_pieces(after(share, slopes, own_near, other_near))
    near = [weights, near]
    other = swap_half(x)
    x_own = after(x, own_split[0], other_split[0])
    z, *_ = project(place, frames, [(x_own, None)], own_blocks, near, 1)
    own_split = prepare(place, after(x, z), x_near)
    far = [*pieces, *map(over_c, after(pieces, own_split[0]))]
    up_away = over_h(after(up_away, other, own_split[0]))
    half_weights.append(near + far)
    z, stats = project(place, frames, [(other, None)], other_blocks, near, 1, z, valid)
    both = jnp.concatenate([own_blocks, other_blocks])
    z_far, stats = project(
        place,
        frames,
        [(x, None), (other, None)],
        both,
        far,
        1,
        None,
        valid,
        stats,
    )
    z = [z, z_far]
    stats = gather(gather(stats, ("y", "x")), ("h", "c"))
    upstream = four_of(up_close, after(up_away, stats))
    *output, states, slopes = recur(1, place, gate, z, stats, params, valid, x, True)
    other_near = over_c(after(other, slopes))
    saved.append((own_split, (other, other_near), z, stats, states, slopes))
    diagonal = over_c(over_h(output[3]))

    ups = upstream
    results = [None] * LAYERS
    for layer in range(LAYERS - 1, -1, -1):
        own_split, other_split, z, stats, states, slopes = saved[layer]
        weight = half_weights[layer]
        grad_pre, sums = back(layer, place, gate, z, stats, params, ups, states, slopes)
        if layer == 0:
            come[0] = after(come[0], sums)
            later, go = step_of((in_hbm(stay[0]), come[0]), (in_hbm(stay[1]), come[1]))
            sums = after(sums, later)
            go = over_second(go)
        sums = gather(gather(sums, ("y", "x")), ("h", "c"))
        if layer > 0:
            away = over_h(after(output[2], sums))
        grad_z, leaving, *terms, sums = norm_back(
            other_columns, place, grad_pre, z, params, valid, stats, sums, weight, layer,
            layer == 0,
        )
        leaving = over_c(leaving)
        if layer > 0:
            received = [swap_half(terms[0])]
            leaving = after(leaving, diagonal)
        else:
            received = [None, swap_half(terms[1])]
            later, go = step_of((later, after(go, grad_z)))
            leaving = after(leaving, later)
            later = (later, over_h(go))
        *first, g_high, g_low = weight_rows(0, place, (grad_z, leaving), own_split, width)
        turned = (g_high, g_low)
        come = [plane_swap(first[1], 0)]
        if layer > 0:
            other_split = prepare(place, *after(other_split, first[0], away))
            output = [(a, 0) for a in (output[0], over_c(output[1]), away, diagonal)]
        else:
            received[0] = swap_half(after(terms[0], received[1]))
        second = weight_rows(1, place, turned, other_split, width)
        come.append(plane_swap(second[1], 0))
        stay = (first[0], second[0])
        kept = own_terms(own_columns, place, after(grad_z, second[0]), ups, weight, layer)
        ups = [(kept, None)] + [(r, None) for r in received]
        results[layer] = lax.dynamic_index_in_dim(
            sums.reshape(3, 4, width), clip, axis=1, keepdims=False
        )

    sums = jnp.stack(results)
    sums = [sums[:, 0], sums[:, 1], sums[:, 2]]
    away = merge(kept, 1, received[1])
    (later,) = step_of((later[0], after(later[1], away)), cut=False)
    away = over_h(away)
    later_first, later_second = plane_swap(later, 0), plane_swap(later, 1)
    come[0] = after(come[0], later_first, sums)
    total, go = step_of((in_hbm(stay[0]), come[0]), (in_hbm(stay[1]), come[1]))
    go = over_second(go)
    later = [later, later_second, later_first, plane_swap(after(later_first, total), 1)]
    far = [(away, 0), (over_c(away), 1)]
    total, go = step_of((total, after(go, far[1][0])))
    go = over_h(go)
    output = unpack(place, [(after(array, total), i) for array, i in output], frames, waited=True)
    grad_weights = assemble(place, after(later, output), 1)
    close = merge(kept, 0, after(received[0], grad_weights))
    (share,) = step_of((total, after(go, close)), cut=False)
    gathered = plane_gather(share)
    grad_in = [(close, 0), (over_c(close[frames:]), 0)] + far
    grad_in = unpack(place, grad_in, frames)
    grad_weights = assemble(place, after(gathered, grad_in), 0, grad_weights)
    return (output, grad_in, grad_weights, *sums, sums[1])


def gelu_slope(value):
    return (
        0.5 * (1.0 + jax.scipy.special.erf(value / ROOT_TWO))
        + value * jnp.exp(-0.5 * value * value) / ROOT_TWO_PI
    )


def recur_step(decay, state, inputs):
    drive_t, valid_t = inputs
    pre = drive_t + decay * state
    state = state + valid_t * (jax.nn.gelu(pre, approximate=False) - state)
    return (state, state)


def back_step(decay, carry, inputs):
    upstream_t, valid_t, pre_t = inputs
    total = upstream_t + carry
    grad_pre = total * valid_t * gelu_slope(pre_t)
    carry = total * (1.0 - valid_t) + grad_pre * decay
    return (carry, grad_pre)


def add_piece(weight, piece):
    return jnp.dot(weight, piece, precision=HIGH, preferred_element_type=jnp.float32)


def weight_columns(grad_pre_norm, piece):
    return jnp.einsum("jf,kf->jk", grad_pre_norm, piece, precision=HIGH)


def split_features(inputs, weights, gains, shifts, decays, biases, lengths, frame_mask, grad_out):
    width, slots = inputs.shape
    clips, frames_len = frame_mask.shape
    frames = jnp.arange(frames_len, dtype=jnp.int32)
    valid_grid = (
        (frames[None, :] < lengths[:, None]) & ((frame_mask == 1) | (frames[None, :] == 0))
    ).astype(jnp.float32)
    valid = valid_grid.reshape(-1)
    valid_row = valid[None, :]
    valid_time = jnp.broadcast_to(valid_grid.T[:, :, None], (frames_len, clips, width)).reshape(
        frames_len, clips * width
    )
    count_local = jnp.sum(valid)

    def to_time(array):
        return jnp.transpose(array.reshape(width, clips, frames_len), (2, 1, 0)).reshape(
            frames_len, clips * width
        )

    def from_time(array):
        return jnp.transpose(array.reshape(frames_len, clips, width), (2, 1, 0)).reshape(
            width, slots
        )

    layer_in = inputs
    saved = []
    for layer_no in range(LAYERS):
        weight = weights[layer_no]
        gathered = lax.all_gather(layer_in, "neuron", axis=0, tiled=True)
        pre_norm = add_piece(weight, gathered)
        first_sum, count = lax.psum((jnp.sum(valid_row * pre_norm, axis=1), count_local), "batch")
        mean = first_sum / count
        centered = pre_norm - mean[:, None]
        var = lax.psum(jnp.sum(valid_row * centered * centered, axis=1), "batch") / count
        inv_std = lax.rsqrt(var + EPS)
        zhat = (pre_norm - mean[:, None]) * inv_std[:, None]
        drive = gains[layer_no][:, None] * zhat + (shifts[layer_no] + biases[layer_no])[:, None]
        drive_time = to_time(drive)
        decay_wide = jnp.tile(decays[layer_no], clips)
        start_state = jnp.zeros((clips * width,), jnp.float32)
        _, states = lax.scan(
            partial(recur_step, decay_wide), start_state, (drive_time, valid_time), unroll=8
        )
        saved.append((gathered, zhat, inv_std, drive_time, states, count))
        layer_in = layer_in + valid_row * from_time(states)
    upstream = grad_out
    grad_parts = [None] * LAYERS
    for layer_no in range(LAYERS - 1, -1, -1):
        gathered, zhat, inv_std, drive_time, states, count = saved[layer_no]
        decay_wide = jnp.tile(decays[layer_no], clips)
        gain = gains[layer_no]
        previous = jnp.concatenate([jnp.zeros_like(states[:1]), states[:-1]], axis=0)
        pre_time = drive_time + decay_wide[None, :] * previous
        grad_state = to_time(valid_row * upstream)
        start_carry = jnp.zeros((clips * width,), jnp.float32)
        _, grad_pre_time = lax.scan(
            partial(back_step, decay_wide),
            start_carry,
            (grad_state, valid_time, pre_time),
            reverse=True,
            unroll=8,
        )
        decay_local = jnp.sum(
            jnp.sum(grad_pre_time * previous, axis=0).reshape(clips, width), axis=0
        )
        grad_pre = from_time(grad_pre_time)
        gain_local = jnp.sum(grad_pre * zhat, axis=1)
        shift_local = jnp.sum(grad_pre, axis=1)
        grad_gain, grad_shift, grad_decay = lax.psum(
            (gain_local, shift_local, decay_local), "batch"
        )
        grad_pre_norm = (gain * inv_std)[:, None] * (
            grad_pre - valid_row * (grad_shift[:, None] + zhat * grad_gain[:, None]) / count
        )
        weight_local = weight_columns(grad_pre_norm, gathered)
        input_terms = jnp.einsum("jk,jf->kf", weights[layer_no], grad_pre_norm, precision=HIGH)
        input_grad = lax.psum_scatter(input_terms, "neuron", scatter_dimension=0, tiled=True)
        grad_weight = lax.psum(weight_local, "batch")
        upstream = upstream + input_grad
        grad_parts[layer_no] = (grad_weight, grad_gain, grad_shift, grad_decay)
    grad_weights = jnp.stack([grad_parts[layer_no][0] for layer_no in range(LAYERS)])
    grad_gains = jnp.stack([grad_parts[layer_no][1] for layer_no in range(LAYERS)])
    grad_shifts = jnp.stack([grad_parts[layer_no][2] for layer_no in range(LAYERS)])
    grad_decays = jnp.stack([grad_parts[layer_no][3] for layer_no in range(LAYERS)])
    return (layer_in, upstream, grad_weights, grad_gains, grad_shifts, grad_decays, grad_shifts)


def solution(mesh):
    if (mesh.shape["batch"], mesh.shape["neuron"]) == (4, 8):
        cut = Mesh(mesh.devices.reshape(2, 2, 2, 2, 2), ("y", "x", "h", "l", "c"))
        batch, neuron, body = ("y", "x"), ("h", "l", "c"), half_features
    else:
        cut, batch, neuron, body = mesh, "batch", "neuron", split_features
    in_specs = (
        P(neuron, batch),
        P(None, neuron, None),
        P(None, neuron),
        P(None, neuron),
        P(None, neuron),
        P(None, neuron),
        P(batch),
        P(batch, None),
        P(neuron, batch),
    )
    out_specs = (
        P(neuron, batch),
        P(neuron, batch),
        P(None, neuron, None),
        P(None, neuron),
        P(None, neuron),
        P(None, neuron),
        P(None, neuron),
    )
    return jax.shard_map(
        body, mesh=cut, in_specs=in_specs, out_specs=out_specs, check_vma=False
    )
```

```python
from functools import partial
import math

import jax
import jax.numpy as jnp
from jax import lax
from jax.experimental import pallas as pl
from jax.experimental.pallas import tpu as pltpu
from jax.sharding import Mesh, PartitionSpec as P

LAYERS = 2
EPS = 1e-05
HIGH = lax.Precision.HIGHEST
ROOT_TWO = math.sqrt(2.0)
ROOT_TWO_PI = math.sqrt(2.0 * math.pi)
F32 = jnp.float32
BF16 = jnp.bfloat16
LANES = 128
VMEM_LIMIT = 24 * 1024 * 1024
SMEM_SPEC = pl.BlockSpec(memory_space=pltpu.SMEM)
VMEM_SPEC = pl.BlockSpec(memory_space=pltpu.VMEM)


FLIP2 = [(0, 1), (1, 0)]
DIAGONAL = [(0, 3), (1, 2), (2, 1), (3, 0)]


def swap_half(array):
    return lax.ppermute(array, "l", FLIP2)


def after(value, *others):
    return lax.optimization_barrier((value, others))[0]


def split(value):
    high = value.astype(BF16)
    return high, (value - high.astype(F32)).astype(BF16)


def dot(a, b, dims):
    return lax.dot_general(a, b, (dims, ((), ())), preferred_element_type=F32)


NT = ((1,), (1,))
NN = ((1,), (0,))


def in_hbm(array):
    return pltpu.with_memory_space_constraint(array, pltpu.HBM)


def call(body, out_shape, hbm_outs=(), **kwargs):
    if hbm_outs:
        out_shape = [
            pltpu.HBM(a.shape, a.dtype) if i in hbm_outs else a for i, a in enumerate(out_shape)
        ]
    return pl.pallas_call(
        body,
        out_shape=out_shape,
        compiler_params=pltpu.CompilerParams(vmem_limit_bytes=VMEM_LIMIT),
        **kwargs,
    )


def cost(flops, byte_count):
    return pl.CostEstimate(flops=int(flops) // 64, bytes_accessed=int(byte_count) // 64, transcendentals=0)


def pack_body(frames, place_ref, in_ref, near_ref, far_ref, turned):
    slots = in_ref.shape[1]
    for start in range(0, slots, LANES):
        turned[start : start + LANES, :] = in_ref[:, start : start + LANES].T
    for rel in range(4):
        first = pl.multiple_of(place_ref[rel] * frames, 8)
        out = (near_ref, far_ref)[rel // 2]
        out[(rel % 2) * frames : (rel % 2 + 1) * frames, :] = turned[pl.ds(first, frames), :]


def pack(place, array, frames, waits=False):
    width, slots = array.shape
    out = jax.ShapeDtypeStruct((2 * frames, width), F32)
    return call(
        partial(pack_body, frames),
        grid=(1,),
        out_shape=[out, out],
        in_specs=[SMEM_SPEC, pl.BlockSpec((width, slots), lambda i: (0, 0))],
        out_specs=[pl.BlockSpec(out.shape, lambda i: (0, 0))] * 2,
        scratch_shapes=[pltpu.VMEM((slots, width), F32)],
        hbm_outs=(0, 1) if waits else (),
        cost_estimate=cost(0, 8 * width * slots),
        name="pack",
    )(place, in_hbm(array))


def part_spec(part, frames):
    array, i = part
    if i is None:
        return pl.BlockSpec(array.shape, lambda *_: (0,) * array.ndim)
    return pl.BlockSpec((frames, array.shape[1]), lambda *_: (i, 0))


def arrays_of(parts):
    return [array for array, _ in parts]


def unpack_body(frames, place_ref, *refs):
    ins, out_ref, turned = refs[:4], refs[4], refs[5]
    slots = out_ref.shape[1]
    for rel in range(4):
        first = pl.multiple_of(place_ref[rel] * frames, 8)
        turned[pl.ds(first, frames), :] = ins[rel][...]
    for start in range(0, slots, LANES):
        out_ref[:, start : start + LANES] = turned[start : start + LANES, :].T


def unpack(place, parts, frames, waited=False):
    width = parts[0][0].shape[1]
    slots = 4 * frames
    return call(
        partial(unpack_body, frames),
        grid=(1,),
        out_shape=jax.ShapeDtypeStruct((width, slots), F32),
        in_specs=[SMEM_SPEC] + [part_spec(part, frames) for part in parts],
        out_specs=pl.BlockSpec((width, slots), lambda i: (0, 0)),
        scratch_shapes=[pltpu.VMEM((slots, width), F32)],
        cost_estimate=cost(0, 8 * width * slots),
        name="unpack",
    )(place, *[in_hbm(a) if waited else a for a in arrays_of(parts)])


def merge_body(kept_ref, come_ref, out_ref):
    frames, columns = kept_ref.shape
    width = columns // 2
    for i in range(2):
        some = slice(i * width, (i + 1) * width)
        out_ref[i * frames : (i + 1) * frames, :] = kept_ref[:, some] + come_ref[:, some]


def merge(kept, half, come):
    frames, columns = come.shape
    return call(
        merge_body,
        grid=(1,),
        out_shape=jax.ShapeDtypeStruct((2 * frames, columns // 2), F32),
        in_specs=[
            pl.BlockSpec((frames, columns), lambda i: (0, half)),
            pl.BlockSpec((frames, columns), lambda i: (0, 0)),
        ],
        out_specs=pl.BlockSpec((2 * frames, columns // 2), lambda i: (0, 0)),
        cost_estimate=cost(0, 12 * frames * columns),
        name="merge",
    )(kept, come)


def project_body(n_parts, n_flat, spots, n_weights, first, with_acc, with_stats, with_params, cols_ref, place_ref, *refs):
    del cols_ref

    def take(n):
        nonlocal refs
        some, refs = refs[:n], refs[n:]
        return some

    parts, flat_parts, weights = take(n_parts), take(n_flat), take(n_weights)
    acc, valid, stats_in, params = take(with_acc), take(with_stats > 0), take(with_stats > 1), take(with_params)
    (out_ref,) = take(1)
    stats, flat = take(with_stats > 0), take(n_flat > 0)
    x_high, x_low, far_ref = refs
    step = pl.program_id(0)
    width = x_high.shape[2]

    @pl.when(step == 0)
    def _():
        for block, part in zip(spots, parts):
            for start in range(0, part.shape[1], width):
                high, low = split(part[:, start : start + width])
                x_high[block + start // width] = high
                x_low[block + start // width] = low
        column = 0
        for part in flat_parts:
            flat[0][:, column : column + part.shape[1]] = part[...]
            column += part.shape[1]
        if with_acc:
            out_ref[...] = acc[0][...]
        else:
            out_ref[...] = jnp.zeros_like(out_ref)

    stacked = jnp.concatenate([x_high[step], x_low[step], x_high[step]], axis=1)
    for block, weight in enumerate(weight_blocks(place_ref, weights, far_ref)):
        w_high, w_low = split(weight)
        columns = slice(block * width, (block + 1) * width)
        out_ref[:, columns] += dot(stacked, jnp.concatenate([w_high, w_high, w_low], axis=1), NT)

    if with_stats:
        (stats_ref,) = stats

        @pl.when(step == pl.num_programs(0) - 1)
        def _():
            if stats_in:
                stats_ref[...] = stats_in[0][...]
            own = jnp.sum(valid[0][...], axis=0, keepdims=True)
            per = width // LANES
            for row in range(out_ref.shape[1] // LANES):
                z = out_ref[:, row * LANES : (row + 1) * LANES]
                total = jnp.sum(valid[0][...] * z, axis=0, keepdims=True)
                centred = valid[0][...] * (z - total / own)
                squares = jnp.sum(centred * centred, axis=0, keepdims=True)
                at = place_ref[first + row // per] * per + row % per
                stats_ref[0, pl.ds(at, 1), :] = total
                stats_ref[1, pl.ds(at, 1), :] = squares
                stats_ref[2, pl.ds(at, 1), :] = own
            if with_params:
                rest = params[0].shape[0] - 8
                stats_ref[3] = params[0][:8, :]
                stats_ref[4] = jnp.zeros_like(stats_ref[4])
                stats_ref[4, :rest, :] = params[0][8:, :]


def weight_specs(weights, layer, pairs=2):
    specs = []
    for weight in weights:
        if weight.ndim == 3:
            shape = (1, weight.shape[1], pairs * weight.shape[1])
            specs.append(pl.BlockSpec(shape, lambda s, cols, *_: (layer, 0, cols[s])))
        else:
            shape = (weight.shape[0], pairs * 4 * weight.shape[0])
            specs.append(pl.BlockSpec(shape, lambda s, cols, *_: (0, cols[s])))
    return specs


def far_scratch(width, pairs=2):
    return pltpu.VMEM((2, width, pairs * width), F32)


def weight_blocks(place_ref, refs, far_ref):
    near = [ref[0] for ref in refs if len(ref.shape) == 3]
    pieces = [ref for ref in refs if len(ref.shape) == 2]
    far = []
    for i in range(len(pieces) // 4):
        for rel, piece in enumerate(pieces[4 * i : 4 * i + 4]):
            rows = piece.shape[0]
            row = 2 * (place_ref[4] ^ (rel // 2)) + (place_ref[5] ^ (rel % 2))
            far_ref[i, pl.ds(pl.multiple_of(row * rows, rows), rows), :] = piece[...]
        far.append(far_ref[i])
    return near + far


def project(
    place, frames, parts, blocks, weights, layer, acc=None, valid=None, stats=None, params=None, flat=()
):
    near = weights[0].ndim == 3
    units = sum(1 if w.ndim == 3 else 0.25 for w in weights)
    width = weights[0].shape[1] if near else 4 * weights[0].shape[0]
    n = blocks.shape[0]
    spots, block = [], 0
    for array, _ in parts:
        spots.append(block)
        block += array.shape[1] // width
    full = pl.BlockSpec(memory_space=pltpu.VMEM)
    in_specs = [part_spec(part, frames) for part in (*parts, *flat)]
    in_specs += weight_specs(weights, layer, 1)
    operands = arrays_of(parts) + arrays_of(flat) + [in_hbm(w) for w in weights]
    array = jax.ShapeDtypeStruct((frames, int(units) * width), F32)
    array_spec = pl.BlockSpec(array.shape, lambda s, cols, place: (0, 0))
    out_shape, out_specs = [array], [array_spec]
    if acc is not None:
        in_specs.append(array_spec)
        operands.append(in_hbm(acc))
    if valid is not None:
        in_specs.append(full)
        operands.append(valid)
        shape = (3 if params is None else 5, 4 * width // LANES, LANES)
        out_shape.append(jax.ShapeDtypeStruct(shape, F32))
        out_specs.append(pl.BlockSpec(shape, lambda s, cols, place: (0, 0, 0)))
    for extra in (stats, params):
        if extra is not None:
            in_specs.append(full)
            operands.append(extra)
    if flat:
        out_shape.append(jax.ShapeDtypeStruct((frames, 4 * width), F32))
        out_specs.append(pl.BlockSpec((frames, 4 * width), lambda s, cols, place: (0, 0)))
    return call(
        partial(
            project_body,
            len(parts),
            len(flat),
            spots,
            len(weights),
            0 if near else 2,
            acc is not None,
            (valid is not None) + (stats is not None),
            params is not None,
        ),
        grid_spec=pltpu.PrefetchScalarGridSpec(
            num_scalar_prefetch=2,
            grid=(n,),
            in_specs=in_specs,
            out_specs=out_specs,
            scratch_shapes=[pltpu.VMEM((n, frames, width), BF16)] * 2 + [far_scratch(width, 1)],
        ),
        out_shape=out_shape,
        hbm_outs=(0, len(out_shape) - 1) if flat else (0,),
        cost_estimate=cost(6 * frames * n * width * units * width, 4 * n * width * units * width),
        name="project",
    )(blocks, place, *operands)


def to_relative(place_ref, spread, rows_ref, value, slot):
    per = value.shape[0] // 4
    spread[...] = value
    for rel in range(4):
        first = place_ref[rel] * per
        for row in range(per):
            rows_ref[slot, rel * per + row : rel * per + row + 1, :] = spread[
                pl.ds(first + row, 1), :
            ]


def tree(values):
    while len(values) > 1:
        values = [a + b for a, b in zip(values[::2], values[1::2])]
    return values[0]


def gathered(ref, slot):
    return [ref[i] for i in range(slot, ref.shape[0], ref.shape[0] // 16)]


def norm_terms(stats_ref):
    each = [gathered(stats_ref, slot) for slot in range(3)]
    totals, squares, owns = each
    count = tree(owns)
    mean = tree(totals) / count
    away = [total / own - mean for total, own in zip(totals, owns)]
    spread = tree([s + n * a * a for s, n, a in zip(squares, owns, away)])
    return count, mean, lax.rsqrt(spread / count + EPS)


CHUNKS = 4


def columns_of(refs, row):
    for ref in refs:
        if row * LANES < ref.shape[1]:
            return ref[:, row * LANES : (row + 1) * LANES]
        row -= ref.shape[1] // LANES


def recur_body(n_z, last, layer, spread_params, place_ref, gate_ref, *refs):
    z_refs, refs = refs[:n_z], refs[n_z:]
    (stats_ref, params_ref, valid_ref, x_ref), refs = refs[:4], refs[4:]
    outs, refs = refs[: 1 + 3 * last], refs[1 + 3 * last :]
    if spread_params:
        state_ref, slope_ref, params_out, rows, spread, held, drive_s, state_s, slope_s = refs
    else:
        state_ref, slope_ref, rows, spread, held, drive_s, state_s, slope_s = refs
    frames, features = x_ref.shape
    blocks = features // LANES
    per = blocks // 4
    chunk = pl.program_id(0)

    @pl.when(chunk == 0)
    def _():
        if spread_params:
            for rel in range(4):
                first = place_ref[rel] * (stats_ref.shape[0] // 16) + 3
                for row in range(LAYERS * 3 * per):
                    at = rel * per + row % per
                    params_out[row // per, at : at + 1, :] = stats_ref[
                        first + row // 8, row % 8 : row % 8 + 1, :
                    ]
            params = [params_out[3 * layer + i] for i in range(3)]
        else:
            params = [params_ref[3 * layer + i] for i in range(3)]
        _, mean, inv_std = norm_terms(stats_ref)
        to_relative(place_ref, spread, rows, mean, 0)
        to_relative(place_ref, spread, rows, inv_std, 1)
        rows[1] = rows[1] * params[0]
        rows[2] = params[1]
        rows[3] = params[2]
        held[...] = jnp.zeros_like(held)

    for row in range(blocks):
        drive_s[row * frames : (row + 1) * frames, :] = (
            columns_of(z_refs, row) - rows[0, row : row + 1, :]
        ) * rows[1, row : row + 1, :] + rows[2, row : row + 1, :]
    decay = rows[3]

    def step(t, state):
        at = pl.ds(t, blocks, stride=frames)
        pre = drive_s[at, :] + decay * state
        half = 0.5 + 0.5 * lax.erf(pre * (1.0 / ROOT_TWO))
        gate = gate_ref[chunk * frames + t] > 0.0
        slope = half + pre * jnp.exp(-0.5 * pre * pre) * (1.0 / ROOT_TWO_PI)
        state = jnp.where(gate, pre * half, state)
        state_s[at, :] = state
        slope_s[at, :] = jnp.where(gate, slope, 0.0)
        return state

    held[...] = lax.fori_loop(0, frames, step, held[...], unroll=8)
    valid = valid_ref[...]
    for row in range(blocks):
        lanes = slice(row * LANES, (row + 1) * LANES)
        state = state_s[row * frames : (row + 1) * frames, :]
        state_ref[:, lanes] = state
        slope_ref[:, lanes] = slope_s[row * frames : (row + 1) * frames, :]
        value = x_ref[:, lanes] + valid * state
        out, at = (outs[row // per], row % per) if last else (outs[0], row)
        out[:, at * LANES : (at + 1) * LANES] = value


def recur(layer, place, gate, z, stats, params, valid, x, last):
    frames, features = x.shape
    blocks = features // LANES
    some = frames // CHUNKS
    whole = lambda array: pl.BlockSpec(array.shape, lambda i: (0,) * array.ndim)
    by_chunk = lambda array: pl.BlockSpec((some, array.shape[1]), lambda i: (i, 0))
    full = jax.ShapeDtypeStruct((frames, features), F32)
    piece = jax.ShapeDtypeStruct((frames, features // 4), F32)
    out_shape = [piece] * 4 if last else [full]
    out_shape += [full, full]
    out_specs = [by_chunk(a) for a in out_shape]
    spread_params = params is None
    if spread_params:
        out_shape.append(jax.ShapeDtypeStruct((3 * LAYERS, blocks, LANES), F32))
        out_specs.append(whole(out_shape[-1]))
        params = valid
    return call(
        partial(recur_body, len(z), last, layer, spread_params),
        grid=(CHUNKS,),
        in_specs=[SMEM_SPEC, SMEM_SPEC]
        + [by_chunk(a) for a in z]
        + [whole(a) for a in (stats, params)]
        + [by_chunk(a) for a in (valid, x)],
        out_specs=out_specs,
        out_shape=out_shape,
        hbm_outs=tuple(range(len(out_shape) - spread_params)) if last else (1, 2),
        scratch_shapes=[
            pltpu.VMEM((4, blocks, LANES), F32),
            pltpu.VMEM((blocks, LANES), F32),
            pltpu.VMEM((blocks, LANES), F32),
        ]
        + [pltpu.VMEM((blocks * some, LANES), F32)] * 3,
        cost_estimate=cost(100 * frames * features, 20 * frames * features),
        name="recur",
    )(place, gate, *[in_hbm(a) for a in z], stats, params, valid, in_hbm(x))


def back_body(n_z, n_ups, spots, layer, place_ref, gate_ref, *refs):
    z_refs, refs = refs[:n_z], refs[n_z:]
    (stats_ref, params_ref), refs = refs[:2], refs[2:]
    ups, (state_ref, slope_ref), refs = refs[:n_ups], refs[n_ups : n_ups + 2], refs[n_ups + 2 :]
    grad_ref, sums_ref, rows, spread, held, up_s, state_s, slope_s = refs
    frames, features = state_ref.shape
    blocks = features // LANES
    per = blocks // 4
    tall = frames + 8
    step_no = pl.program_id(0)
    chunk = pl.num_programs(0) - 1 - step_no

    @pl.when(step_no == 0)
    def _():
        _, mean, inv_std = norm_terms(stats_ref)
        to_relative(place_ref, spread, rows, mean, 0)
        to_relative(place_ref, spread, rows, inv_std, 1)
        held[...] = jnp.zeros_like(held)

    for row in range(blocks):
        lanes = slice(row * LANES, (row + 1) * LANES)
        base = row * frames
        up = None
        for (_, column), part in zip(spots, ups):
            if column <= row * LANES < column + part.shape[1]:
                value = part[:, row * LANES - column : (row + 1) * LANES - column]
                up = value if up is None else up + value
        up_s[base : base + frames, :] = up
        state_s[row * tall : row * tall + 8, :] = jnp.zeros((8, LANES), F32)
        state_s[row * tall + 8 : (row + 1) * tall, :] = state_ref[:, lanes]
        slope_s[base : base + frames, :] = slope_ref[:, lanes]
    decay = params_ref[3 * layer + 2]

    def step(i, carry):
        t = frames - 1 - i
        at = pl.ds(t, blocks, stride=frames)
        slope = slope_s[at, :]
        gate = gate_ref[chunk * frames + t]
        total = gate * up_s[at, :] + carry
        up_s[at, :] = total * slope
        return total * (slope * decay + (1.0 - gate))

    held[0] = lax.fori_loop(0, frames, step, held[0], unroll=8)
    held[4] += held[1] * state_s[pl.ds(tall - 1, blocks, stride=tall), :]
    held[1] = up_s[pl.ds(0, blocks, stride=frames), :]
    for row in range(blocks):
        lanes = slice(row * LANES, (row + 1) * LANES)
        grad = up_s[row * frames : (row + 1) * frames, :]
        grad_ref[:, lanes] = grad
        zhat = (columns_of(z_refs, row) - rows[0, row : row + 1, :]) * rows[1, row : row + 1, :]
        before = state_s[row * tall + 7 : row * tall + 7 + frames, :]
        for slot, value in enumerate((grad * zhat, grad, grad * before)):
            held[2 + slot, row : row + 1, :] += jnp.sum(value, axis=0, keepdims=True)

    @pl.when(chunk == 0)
    def _():
        for row in range(blocks):
            at = place_ref[row // per] * per + row % per
            for slot in range(3):
                sums_ref[slot, pl.ds(at, 1), :] = held[2 + slot, row : row + 1, :]


def spots_of_sum(parts, width):
    spots, column = [], 0
    for array, _ in parts:
        spots.append((0, column % (4 * width)))
        column += array.shape[1]
    return spots


def back(layer, place, gate, z, stats, params, ups, states, slopes):
    frames, features = states.shape
    width = features // 4
    blocks = features // LANES
    some = frames // CHUNKS
    whole = lambda array: pl.BlockSpec(array.shape, lambda i: (0,) * array.ndim)

    def by_chunk(array, first=0):
        return pl.BlockSpec(
            (some, array.shape[1]), lambda i: ((first or 0) * CHUNKS + CHUNKS - 1 - i, 0)
        )

    out_shape = [
        jax.ShapeDtypeStruct((frames, features), F32),
        jax.ShapeDtypeStruct((3, blocks, LANES), F32),
    ]
    return call(
        partial(back_body, len(z), len(ups), spots_of_sum(ups, width), layer),
        grid=(CHUNKS,),
        in_specs=[SMEM_SPEC] * 2
        + [by_chunk(a) for a in z]
        + [whole(a) for a in (stats, params)]
        + [by_chunk(*up) for up in ups]
        + [by_chunk(a) for a in (states, slopes)],
        out_specs=[by_chunk(out_shape[0]), whole(out_shape[1])],
        out_shape=out_shape,
        scratch_shapes=[
            pltpu.VMEM((2, blocks, LANES), F32),
            pltpu.VMEM((blocks, LANES), F32),
            pltpu.VMEM((5, blocks, LANES), F32),
            pltpu.VMEM((blocks * some, LANES), F32),
            pltpu.VMEM((blocks * (some + 8), LANES), F32),
            pltpu.VMEM((blocks * some, LANES), F32),
        ],
        cost_estimate=cost(30 * frames * features, 20 * frames * features),
        name="back",
    )(
        place,
        gate,
        *[in_hbm(a) for a in z],
        stats,
        params,
        *arrays_of(ups),
        in_hbm(states),
        in_hbm(slopes),
    )


def input_terms(high_s, low_s, weights):
    left, right = [], []
    for block, weight in enumerate(weights):
        w_high, w_low = split(weight)
        left += [high_s[block], low_s[block], high_s[block]]
        right += [w_high, w_high, w_low]
    return dot(jnp.concatenate(left, axis=1), jnp.concatenate(right, axis=0), NN)


def norm_back_body(n_z, split_terms, layer, cols_ref, place_ref, grad_ref, *refs):
    del cols_ref
    z_refs, refs = refs[:n_z], refs[n_z:]
    params_ref, valid_ref, stats_ref, sums_ref, *refs = refs
    weights, refs = refs[:10], refs[10:]
    if split_terms:
        out_ref, leave_ref, near_term_ref, far_term_ref, sums_out_ref, *refs = refs
        term_refs, starts = (far_term_ref, near_term_ref), (0, 0)
    else:
        out_ref, leave_ref, term_ref, sums_out_ref, *refs = refs
        term_refs, starts = (term_ref, term_ref), (2 * grad_ref.shape[1] // 4, 0)
    rows, spread, high_s, low_s, far_ref = refs
    blocks = grad_ref.shape[1] // LANES
    width = high_s.shape[2]
    per = width // LANES

    @pl.when(pl.program_id(0) == 0)
    def _():
        count, mean, inv_std = norm_terms(stats_ref)
        to_relative(place_ref, spread, rows, mean, 0)
        to_relative(place_ref, spread, rows, inv_std, 1)
        rows[2] = rows[1] * params_ref[3 * layer]
        sums = [tree(gathered(sums_ref, slot)) for slot in range(3)]
        for slot in range(3):
            sums_out_ref[slot] = sums[slot]
        to_relative(place_ref, spread, rows, sums[0] / count, 3)
        to_relative(place_ref, spread, rows, sums[1] / count, 4)
        valid = valid_ref[...]
        for row in range(blocks):
            lanes = slice(row * LANES, (row + 1) * LANES)
            one = lambda slot: rows[slot, row : row + 1, :]
            zhat = (columns_of(z_refs, row) - one(0)) * one(1)
            value = one(2) * (grad_ref[:, lanes] - valid * (one(4) + zhat * one(3)))
            out_ref[:, lanes] = value
            if (row // per) % 2:
                at = (row // per // 2) * width + (row % per) * LANES
                leave_ref[:, at : at + LANES] = value
            high, low = split(value)
            inner = slice((row % per) * LANES, (row % per + 1) * LANES)
            high_s[row // per, :, inner] = high
            low_s[row // per, :, inner] = low

    value = input_terms(high_s, low_s, weight_blocks(place_ref, weights, far_ref))
    for step, (term_ref, first) in enumerate(zip(term_refs, starts)):

        @pl.when(pl.program_id(0) == step)
        def _():
            for pair in range(2):
                at = pl.multiple_of(((place_ref[0] & 1) ^ pair) * width, width)
                term_ref[:, pl.ds(first + at, width)] = value[
                    :, pair * width : (pair + 1) * width
                ]


def norm_back(columns, place, grad, z, params, valid, stats, sums, weights, layer, split_terms):
    frames, features = grad.shape
    width = features // 4
    blocks = features // LANES
    whole = lambda array: pl.BlockSpec(array.shape, lambda s, cols, place: (0,) * array.ndim)
    operands = [grad, *[in_hbm(a) for a in z], params, valid, stats, sums]
    full = jax.ShapeDtypeStruct((frames, features), F32)
    half = jax.ShapeDtypeStruct((frames, 2 * width), F32)
    terms = [half, half] if split_terms else [full]
    out_shape = [full, half, *terms, jax.ShapeDtypeStruct((3, blocks, LANES), F32)]
    return call(
        partial(norm_back_body, len(z), split_terms, layer),
        grid_spec=pltpu.PrefetchScalarGridSpec(
            num_scalar_prefetch=2,
            grid=(2,),
            in_specs=[whole(a) for a in operands] + weight_specs(weights, layer),
            out_specs=[whole(a) for a in out_shape],
            scratch_shapes=[
                pltpu.VMEM((5, blocks, LANES), F32),
                pltpu.VMEM((blocks, LANES), F32),
                pltpu.VMEM((4, frames, width), BF16),
                pltpu.VMEM((4, frames, width), BF16),
                far_scratch(width),
            ],
        ),
        out_shape=out_shape,
        hbm_outs=(0,),
        cost_estimate=cost(6 * frames * features * features, 4 * features * features),
        name="norm_back",
    )(columns, place, *operands, *[in_hbm(w) for w in weights])


def own_terms_body(n_ups, spots, cols_ref, place_ref, grad_ref, *refs):
    del cols_ref
    ups, refs = refs[:n_ups], refs[n_ups:]
    weights, refs = refs[:10], refs[10:]
    out_ref, high_s, low_s, far_ref = refs
    width = high_s.shape[2]
    step = pl.program_id(0)

    @pl.when(step == 0)
    def _():
        for block in range(4):
            high, low = split(grad_ref[:, block * width : (block + 1) * width])
            high_s[block] = high
            low_s[block] = low

    value = input_terms(high_s, low_s, weight_blocks(place_ref, weights, far_ref))
    for pair in range(2):
        at = pl.multiple_of(((place_ref[0] & 1) ^ pair) * width, width)
        out_ref[:, pl.ds(at, width)] = value[:, pair * width : (pair + 1) * width]
    for half in range(2):

        @pl.when(step == half)
        def _():
            first = 2 * half * width
            for (_, column), up in zip(spots, ups):
                low = max(column, first)
                high = min(column + up.shape[1], first + 2 * width)
                if low < high:
                    out_ref[:, low - first : high - first] += up[:, low - column : high - column]


def own_terms(columns, place, grad, ups, weights, layer):
    frames, features = grad.shape
    width = features // 4
    whole = lambda array: pl.BlockSpec(array.shape, lambda s, cols, place: (0,) * array.ndim)
    step_block = pl.BlockSpec((frames, 2 * width), lambda s, cols, place: (0, s))
    return call(
        partial(own_terms_body, len(ups), spots_of_sum(ups, width)),
        grid_spec=pltpu.PrefetchScalarGridSpec(
            num_scalar_prefetch=2,
            grid=(2,),
            in_specs=[whole(grad)]
            + [part_spec(up, frames) for up in ups]
            + weight_specs(weights, layer),
            out_specs=step_block,
            scratch_shapes=[pltpu.VMEM((4, frames, width), BF16)] * 2 + [far_scratch(width)],
        ),
        out_shape=jax.ShapeDtypeStruct((frames, features), F32),
        cost_estimate=cost(6 * frames * features * features, 4 * features * features),
        name="own_terms",
    )(columns, place, in_hbm(grad), *arrays_of(ups), *[in_hbm(w) for w in weights])


def prepare_body(lists_ref, place_ref, own_ref, near_ref, high_ref, low_ref):
    del lists_ref
    padded = high_ref.shape[0] // 2
    width = high_ref.shape[1] // 2
    for clip, part in enumerate((own_ref, near_ref)):
        rows = part.shape[0]
        for dc in range(2):
            at = pl.multiple_of((place_ref[6] ^ clip ^ dc) * width, width)
            high, low = split(part[:, dc * width : (dc + 1) * width])
            high_ref[clip * padded : clip * padded + rows, pl.ds(at, width)] = high
            low_ref[clip * padded : clip * padded + rows, pl.ds(at, width)] = low
        zeros = jnp.zeros((padded - rows, 2 * width), BF16)
        high_ref[clip * padded + rows : (clip + 1) * padded, :] = zeros
        low_ref[clip * padded + rows : (clip + 1) * padded, :] = zeros


def prepare(place, own, near):
    frames, features = own.shape
    width = features // 4
    padded = -(-frames // LANES) * LANES
    in_spec = pl.BlockSpec((frames, 2 * width), lambda s, *_: (0, s))
    out = jax.ShapeDtypeStruct((2 * padded, features), BF16)
    out_spec = pl.BlockSpec((2 * padded, 2 * width), lambda s, order, place: (0, order[s]))
    order = jnp.stack([place[0] >> 1, 1 - (place[0] >> 1)])
    return call(
        prepare_body,
        grid_spec=pltpu.PrefetchScalarGridSpec(
            num_scalar_prefetch=2,
            grid=(2,),
            in_specs=[in_spec, in_spec],
            out_specs=[out_spec, out_spec],
        ),
        out_shape=[out, out],
        hbm_outs=(0, 1),
        cost_estimate=cost(0, 16 * frames * features),
        name="prepare",
    )(order, place, in_hbm(own), in_hbm(near))


def product(g_high, g_low, x_high, x_low):
    return dot(g_high, x_high, NN) + (dot(g_high, x_low, NN) + dot(g_low, x_high, NN))


def weight_body(turn, place_ref, *refs):
    if turn:
        grad_ref, near_ref, x_high, x_low, kept, sent, g_high, g_low, t_high, t_low = refs

        @pl.when(pl.program_id(0) == 0)
        def _():
            frames, features = grad_ref.shape
            width = features // 4
            rows = width // 4
            padded = t_high.shape[1] // 2
            t_high[...] = jnp.zeros_like(t_high)
            t_low[...] = jnp.zeros_like(t_low)
            for clip in range(2):
                for dh in range(2):
                    if clip == 0:
                        part = grad_ref[:, 2 * dh * width : (2 * dh + 1) * width]
                    else:
                        part = near_ref[:, dh * width : (dh + 1) * width]
                    high, low = split(part.T)
                    at = (
                        slice(dh * width, (dh + 1) * width),
                        slice(clip * padded, clip * padded + frames),
                    )
                    t_high[at] = high
                    t_low[at] = low
            for group in range(8):
                first, second, dh = group // 4, group // 2 % 2, group % 2
                core = place_ref[6]
                y = place_ref[4] ^ (first * core + second * (1 - core))
                x = place_ref[5] ^ (first * (1 - core) + second * core)
                at = pl.multiple_of(dh * width + (2 * y + x) * rows, rows)
                g_high[group * rows : (group + 1) * rows, :] = t_high[pl.ds(at, rows), :]
                g_low[group * rows : (group + 1) * rows, :] = t_low[pl.ds(at, rows), :]

    else:
        g_high, g_low, x_high, x_low, kept, sent = refs
    half = g_high.shape[0] // 2
    value = product(g_high[...], g_low[...], x_high[...], x_low[...])
    kept[...] = value[:half].reshape(kept.shape)
    sent[...] = value[half:].reshape(sent.shape)


def weight_rows(side, place, grads, x_split, width):
    turn = side == 0
    whole = lambda array: pl.BlockSpec(array.shape, lambda s, place: (0,) * array.ndim)
    x_spec = pl.BlockSpec((x_split[0].shape[0], width), lambda s, place: (0, s))
    shape = (2, 2, width // 4, 4 * width)
    out_shape = [jax.ShapeDtypeStruct(shape, F32)] * 2
    out_specs = [pl.BlockSpec(shape[:3] + (width,), lambda s, place: (0, 0, 0, s))] * 2
    scratch = []
    if turn:
        turned = (2 * width, x_split[0].shape[0])
        out_shape += [jax.ShapeDtypeStruct(turned, BF16)] * 2
        out_specs += [whole(out_shape[-1])] * 2
        scratch = [pltpu.VMEM(turned, BF16)] * 2
    return call(
        partial(weight_body, turn),
        grid_spec=pltpu.PrefetchScalarGridSpec(
            num_scalar_prefetch=1,
            grid=(4,),
            in_specs=[whole(a) for a in grads] + [x_spec] * 2,
            out_specs=out_specs,
            scratch_shapes=scratch,
        ),
        out_shape=out_shape,
        hbm_outs=(0,),
        cost_estimate=cost(12 * x_split[0].shape[0] * width * 4 * width, 4 * 8 * width * width),
        name="weight_rows",
    )(place, *([in_hbm(grads[0]), grads[1]] if turn else grads), *[in_hbm(x) for x in x_split])


def step_body(n, widths, cut, *refs):
    ins, outs = refs[: 2 * n], refs[2 * n :]
    starts = [sum(widths[:i]) for i in range(len(widths))]
    column = 0
    for i in range(n):
        total = ins[2 * i][...] + ins[2 * i + 1][...]
        end = column + total.shape[-1]
        for j, (start, columns) in enumerate(zip(starts, widths)):
            low, high = max(start, column), min(start + columns, end)
            if low < high:
                to = (Ellipsis, slice(low - start, high - start))
                piece = total[..., low - column : high - column]
                if cut:
                    outs[2 * j][to] = piece[0]
                    outs[2 * j + 1][to] = piece[1]
                else:
                    outs[j][to] = piece
        column = end


def step_of(*pairs, cut=True, widths=None):
    shape = list(pairs[0][0].shape)
    widths = widths or [sum(pair[0].shape[-1] for pair in pairs)]
    outs = []
    for columns in widths:
        shape[-1] = columns
        out = jax.ShapeDtypeStruct(tuple(shape[1:] if cut else shape), F32)
        outs += [out] * (1 + cut)
    whole = lambda array: pl.BlockSpec(array.shape, lambda i: (0,) * array.ndim)
    operands = [array for pair in pairs for array in pair]
    return call(
        partial(step_body, len(pairs), widths, cut),
        grid=(1,),
        in_specs=[whole(a) for a in operands],
        out_specs=[whole(a) for a in outs],
        out_shape=outs,
        cost_estimate=cost(0, 4 * sum(a.size for a in operands)),
        name="reduction_step",
    )(*operands)


def plane_swap(array, step):
    pairs = []
    for i in range(8):
        over_x = (i % 2 == 0) == (step == 0)
        pairs.append((i, i ^ 2 if over_x else i ^ 4))
    return lax.ppermute(array, ("y", "x", "c"), pairs)


def plane_gather(share, *before):
    first = plane_swap(share, 0)
    second = plane_swap(share, 1)
    return [share, second, first, plane_swap(after(first, *before), 1)]


def assemble_body(place_ref, *refs):
    out_ref = refs[-1]
    core = place_ref[6]
    rows, columns = refs[0].shape
    quarter = columns // 4
    for i in range(4):
        first, second = i // 2, i % 2
        y = place_ref[4] ^ (first * core + second * (1 - core))
        x = place_ref[5] ^ (first * (1 - core) + second * core)
        at = pl.multiple_of((2 * y + x) * rows, rows)
        for side in range(2):
            for h in range(2):
                to = pl.multiple_of((2 * h + (place_ref[7] ^ side)) * quarter, quarter)
                some = slice((2 * side + h) * quarter, (2 * side + h + 1) * quarter)
                out_ref[0, pl.ds(at, rows), pl.ds(to, quarter)] = refs[i][:, some]


def assemble(place, pieces, layer, onto=None):
    rows, columns = 4 * pieces[0].shape[0], pieces[0].shape[1]
    aliases, extra, extra_specs = {}, [], []
    if onto is not None:
        aliases, extra = {1 + len(pieces): 0}, [onto]
        extra_specs = [pl.BlockSpec(memory_space=pl.ANY)]
    (out,) = call(
        assemble_body,
        grid=(1,),
        out_shape=[jax.ShapeDtypeStruct((LAYERS, rows, columns), F32)],
        hbm_outs=(0,),
        in_specs=[SMEM_SPEC]
        + [pl.BlockSpec(p.shape, lambda i: (0, 0)) for p in pieces]
        + extra_specs,
        out_specs=[pl.BlockSpec((1, rows, columns), lambda i: (layer, 0, 0))],
        input_output_aliases=aliases,
        cost_estimate=cost(0, 8 * rows * columns),
        name="assemble",
    )(place, *[p if extra else in_hbm(p) for p in pieces], *extra)
    return out


def half_features(inputs, weights, gains, shifts, decays, biases, lengths, frame_mask, grad_out):
    width, slots = inputs.shape
    clips, frames = frame_mask.shape
    depth = weights.shape[2]
    blocks = 4 * width // LANES
    y, x, h, l, c = (lax.axis_index(name) for name in ("y", "x", "h", "l", "c"))
    b = 2 * y + x
    numbers = [2 * (h ^ (rel // 2)) + (c ^ (rel % 2)) for rel in range(4)] + [y, x, c, l]
    place = jnp.stack(numbers).astype(jnp.int32)
    own_blocks, other_blocks = (
        jnp.stack(
            [2 * (2 * (h ^ (rel // 2)) + half) + (c ^ (rel % 2)) for rel in range(4)]
        ).astype(jnp.int32)
        for half in (l, 1 - l)
    )
    own_columns = jnp.stack([2 * h + l, 2 * (1 - h) + l]).astype(jnp.int32)
    other_columns = jnp.stack([2 * (1 - h) + 1 - l, 2 * h + 1 - l]).astype(jnp.int32)
    rows = width // 4

    clip = 2 * h + c
    seen = lax.dynamic_index_in_dim(frame_mask, clip, 0, keepdims=False)
    length = lax.dynamic_index_in_dim(lengths, clip, 0, keepdims=False)
    moments = jnp.arange(frames, dtype=jnp.int32)
    gate = ((moments < length) & ((seen == 1) | (moments == 0))).astype(F32)
    valid = jnp.broadcast_to(gate[:, None], (frames, LANES))

    def far_share(layer):
        return lax.dynamic_slice(weights, (layer, b * rows, 0), (1, rows, depth))[0]

    def over_h(array):
        return lax.ppermute(array, "h", FLIP2)

    def over_c(array):
        return lax.ppermute(array, "c", FLIP2)

    def over_second(array):
        return plane_swap(array, 1)

    def four_of(near_rows, far_rows):
        return [
            (near_rows, 0),
            (over_c(near_rows), 1),
            (far_rows, 0),
            (over_c(far_rows), 1),
        ]

    def far_pieces(share):
        both = lax.ppermute(share, ("y", "x"), DIAGONAL)
        return [share, lax.ppermute(share, "x", FLIP2), lax.ppermute(share, "y", FLIP2), both]

    near = over_c(weights)
    share = far_share(0)
    close, away = pack(place, after(inputs, share), frames)
    share = over_h(share)
    away = over_h(away)
    other_close = swap_half(close)
    up_close, up_away = pack(place, after(grad_out, close), frames, waits=True)
    share = after(share, up_close, valid, near, other_close)
    pieces = far_pieces(share)
    away = after(away, pieces[1:])
    half_weights = [[weights, near, *pieces, *map(over_c, after(pieces, away))]]
    own = four_of(after(close, away), away)
    other_away = swap_half(away)
    others = [(other_close, 0), (over_c(other_close), 1)]
    params = jnp.stack([gains, shifts + biases, decays], axis=1)
    own_params = params.reshape(LAYERS * 3 * width // LANES, LANES)
    params = None

    def gather(array, axes):
        return lax.all_gather(array, axes, tiled=True)

    weight = half_weights[0]
    early = jnp.concatenate([own_blocks, other_blocks[:2]])
    z, own_flat = project(place, frames, own + others, early, weight, 0, flat=own)
    others += [(other_away, 0), (over_c(after(other_away, z)), 1)]
    z, stats, other_flat = project(
        place,
        frames,
        others[2:],
        other_blocks[2:],
        weight,
        0,
        z,
        valid,
        params=own_params,
        flat=others,
    )
    z = [z]
    stats = gather(stats, ("h", "c"))
    share = over_c(lax.ppermute(after(far_share(1), stats), ("h", "c"), DIAGONAL))
    stats = gather(stats, ("y", "x"))
    x, states, slopes, params = recur(0, place, gate, z, stats, None, valid, own_flat, False)
    own_near, other_near = over_c(after(own_flat, z[0])), over_c(after(other_flat, z[0]))
    x_near = over_c(x)
    own_split = prepare(place, after(own_flat, x_near), own_near)
    other_split = prepare(place, after(other_flat, x_near), other_near)
    saved = [(own_split, other_split, z, stats, states, slopes)]

    pieces = far_pieces(after(share, slopes, own_near, other_near))
    near = [weights, near]
    other = swap_half(x)
    x_own = after(x, own_split[0], other_split[0])
    z, *_ = project(place, frames, [(x_own, None)], own_blocks, near, 1)
    own_split = prepare(place, after(x, z), x_near)
    far = [*pieces, *map(over_c, after(pieces, own_split[0]))]
    up_away = over_h(after(up_away, other, own_split[0]))
    half_weights.append(near + far)
    z, stats = project(place, frames, [(other, None)], other_blocks, near, 1, z, valid)
    both = jnp.concatenate([own_blocks, other_blocks])
    z_far, stats = project(
        place,
        frames,
        [(x, None), (other, None)],
        both,
        far,
        1,
        None,
        valid,
        stats,
    )
    z = [z, z_far]
    stats = gather(gather(stats, ("y", "x")), ("h", "c"))
    upstream = four_of(up_close, after(up_away, stats))
    *output, states, slopes = recur(1, place, gate, z, stats, params, valid, x, True)
    other_near = over_c(after(other, slopes))
    saved.append((own_split, (other, other_near), z, stats, states, slopes))
    diagonal = over_c(over_h(output[3]))

    ups = upstream
    results = [None] * LAYERS
    for layer in range(LAYERS - 1, -1, -1):
        own_split, other_split, z, stats, states, slopes = saved[layer]
        weight = half_weights[layer]
        grad_pre, sums = back(layer, place, gate, z, stats, params, ups, states, slopes)
        sums = gather(sums, ("y", "x"))
        if layer == 0:
            come[0] = after(come[0], sums)
            later, go = step_of((in_hbm(stay[0]), come[0]), (in_hbm(stay[1]), come[1]))
            sums = after(sums, later)
            go = over_second(go)
        sums = gather(sums, ("h", "c"))
        if layer > 0:
            away = over_h(after(output[2], sums))
        grad_z, leaving, *terms, sums = norm_back(
            other_columns, place, grad_pre, z, params, valid, stats, sums, weight, layer,
            layer == 0,
        )
        leaving = over_c(leaving)
        if layer > 0:
            received = [swap_half(terms[0])]
            other_split = prepare(place, *after(other_split, grad_z))
            leaving = after(leaving, diagonal, other_split[0])
        else:
            received = [None, swap_half(terms[1])]
            later, go = step_of((later, after(go, grad_z)))
            leaving = after(leaving, later)
            later = (later, over_h(go))
        *first, g_high, g_low = weight_rows(0, place, (grad_z, leaving), own_split, width)
        turned = (g_high, g_low)
        come = [plane_swap(first[1], 0)]
        if layer > 0:
            turned = after(turned, away)
            output = [(a, 0) for a in (output[0], over_c(output[1]), away, diagonal)]
        else:
            received[0] = swap_half(after(terms[0], received[1]))
        second = weight_rows(1, place, turned, other_split, width)
        come.append(plane_swap(second[1], 0))
        stay = (first[0], second[0])
        kept = own_terms(own_columns, place, after(grad_z, second[0]), ups, weight, layer)
        ups = [(kept, None)] + [(r, None) for r in received]
        results[layer] = lax.dynamic_index_in_dim(
            sums.reshape(3, 4, width), clip, axis=1, keepdims=False
        )

    sums = jnp.stack(results)
    sums = [sums[:, 0], sums[:, 1], sums[:, 2]]
    away = merge(kept, 1, received[1])
    (later,) = step_of((later[0], after(later[1], away)), cut=False)
    away = over_h(away)
    later_first, later_second = plane_swap(later, 0), plane_swap(later, 1)
    come[0] = after(come[0], later_first, sums)
    total, go = step_of((in_hbm(stay[0]), come[0]), (in_hbm(stay[1]), come[1]))
    go = over_second(go)
    later = [later, later_second, later_first, plane_swap(after(later_first, total), 1)]
    far = [(away, 0), (over_c(away), 1)]
    total, go = step_of((total, after(go, far[1][0])))
    go = over_h(go)
    output = unpack(place, [(after(array, total), i) for array, i in output], frames, waited=True)
    grad_weights = assemble(place, after(later, output), 1)
    close = merge(kept, 0, after(received[0], grad_weights))
    (share,) = step_of((total, after(go, close)), cut=False)
    gathered = plane_gather(share)
    grad_in = [(close, 0), (over_c(close[frames:]), 0)] + far
    grad_in = unpack(place, grad_in, frames)
    grad_weights = assemble(place, after(gathered, grad_in), 0, grad_weights)
    return (output, grad_in, grad_weights, *sums, sums[1])


def gelu_slope(value):
    return (
        0.5 * (1.0 + jax.scipy.special.erf(value / ROOT_TWO))
        + value * jnp.exp(-0.5 * value * value) / ROOT_TWO_PI
    )


def recur_step(decay, state, inputs):
    drive_t, valid_t = inputs
    pre = drive_t + decay * state
    state = state + valid_t * (jax.nn.gelu(pre, approximate=False) - state)
    return (state, state)


def back_step(decay, carry, inputs):
    upstream_t, valid_t, pre_t = inputs
    total = upstream_t + carry
    grad_pre = total * valid_t * gelu_slope(pre_t)
    carry = total * (1.0 - valid_t) + grad_pre * decay
    return (carry, grad_pre)


def add_piece(weight, piece):
    return jnp.dot(weight, piece, precision=HIGH, preferred_element_type=jnp.float32)


def weight_columns(grad_pre_norm, piece):
    return jnp.einsum("jf,kf->jk", grad_pre_norm, piece, precision=HIGH)


def split_features(inputs, weights, gains, shifts, decays, biases, lengths, frame_mask, grad_out):
    width, slots = inputs.shape
    clips, frames_len = frame_mask.shape
    frames = jnp.arange(frames_len, dtype=jnp.int32)
    valid_grid = (
        (frames[None, :] < lengths[:, None]) & ((frame_mask == 1) | (frames[None, :] == 0))
    ).astype(jnp.float32)
    valid = valid_grid.reshape(-1)
    valid_row = valid[None, :]
    valid_time = jnp.broadcast_to(valid_grid.T[:, :, None], (frames_len, clips, width)).reshape(
        frames_len, clips * width
    )
    count_local = jnp.sum(valid)

    def to_time(array):
        return jnp.transpose(array.reshape(width, clips, frames_len), (2, 1, 0)).reshape(
            frames_len, clips * width
        )

    def from_time(array):
        return jnp.transpose(array.reshape(frames_len, clips, width), (2, 1, 0)).reshape(
            width, slots
        )

    layer_in = inputs
    saved = []
    for layer_no in range(LAYERS):
        weight = weights[layer_no]
        gathered = lax.all_gather(layer_in, "neuron", axis=0, tiled=True)
        pre_norm = add_piece(weight, gathered)
        first_sum, count = lax.psum((jnp.sum(valid_row * pre_norm, axis=1), count_local), "batch")
        mean = first_sum / count
        centered = pre_norm - mean[:, None]
        var = lax.psum(jnp.sum(valid_row * centered * centered, axis=1), "batch") / count
        inv_std = lax.rsqrt(var + EPS)
        zhat = (pre_norm - mean[:, None]) * inv_std[:, None]
        drive = gains[layer_no][:, None] * zhat + (shifts[layer_no] + biases[layer_no])[:, None]
        drive_time = to_time(drive)
        decay_wide = jnp.tile(decays[layer_no], clips)
        start_state = jnp.zeros((clips * width,), jnp.float32)
        _, states = lax.scan(
            partial(recur_step, decay_wide), start_state, (drive_time, valid_time), unroll=8
        )
        saved.append((gathered, zhat, inv_std, drive_time, states, count))
        layer_in = layer_in + valid_row * from_time(states)
    upstream = grad_out
    grad_parts = [None] * LAYERS
    for layer_no in range(LAYERS - 1, -1, -1):
        gathered, zhat, inv_std, drive_time, states, count = saved[layer_no]
        decay_wide = jnp.tile(decays[layer_no], clips)
        gain = gains[layer_no]
        previous = jnp.concatenate([jnp.zeros_like(states[:1]), states[:-1]], axis=0)
        pre_time = drive_time + decay_wide[None, :] * previous
        grad_state = to_time(valid_row * upstream)
        start_carry = jnp.zeros((clips * width,), jnp.float32)
        _, grad_pre_time = lax.scan(
            partial(back_step, decay_wide),
            start_carry,
            (grad_state, valid_time, pre_time),
            reverse=True,
            unroll=8,
        )
        decay_local = jnp.sum(
            jnp.sum(grad_pre_time * previous, axis=0).reshape(clips, width), axis=0
        )
        grad_pre = from_time(grad_pre_time)
        gain_local = jnp.sum(grad_pre * zhat, axis=1)
        shift_local = jnp.sum(grad_pre, axis=1)
        grad_gain, grad_shift, grad_decay = lax.psum(
            (gain_local, shift_local, decay_local), "batch"
        )
        grad_pre_norm = (gain * inv_std)[:, None] * (
            grad_pre - valid_row * (grad_shift[:, None] + zhat * grad_gain[:, None]) / count
        )
        weight_local = weight_columns(grad_pre_norm, gathered)
        input_terms = jnp.einsum("jk,jf->kf", weights[layer_no], grad_pre_norm, precision=HIGH)
        input_grad = lax.psum_scatter(input_terms, "neuron", scatter_dimension=0, tiled=True)
        grad_weight = lax.psum(weight_local, "batch")
        upstream = upstream + input_grad
        grad_parts[layer_no] = (grad_weight, grad_gain, grad_shift, grad_decay)
    grad_weights = jnp.stack([grad_parts[layer_no][0] for layer_no in range(LAYERS)])
    grad_gains = jnp.stack([grad_parts[layer_no][1] for layer_no in range(LAYERS)])
    grad_shifts = jnp.stack([grad_parts[layer_no][2] for layer_no in range(LAYERS)])
    grad_decays = jnp.stack([grad_parts[layer_no][3] for layer_no in range(LAYERS)])
    return (layer_in, upstream, grad_weights, grad_gains, grad_shifts, grad_decays, grad_shifts)


def solution(mesh):
    if (mesh.shape["batch"], mesh.shape["neuron"]) == (4, 8):
        cut = Mesh(mesh.devices.reshape(2, 2, 2, 2, 2), ("y", "x", "h", "l", "c"))
        batch, neuron, body = ("y", "x"), ("h", "l", "c"), half_features
    else:
        cut, batch, neuron, body = mesh, "batch", "neuron", split_features
    in_specs = (
        P(neuron, batch),
        P(None, neuron, None),
        P(None, neuron),
        P(None, neuron),
        P(None, neuron),
        P(None, neuron),
        P(batch),
        P(batch, None),
        P(neuron, batch),
    )
    out_specs = (
        P(neuron, batch),
        P(neuron, batch),
        P(None, neuron, None),
        P(None, neuron),
        P(None, neuron),
        P(None, neuron),
        P(None, neuron),
    )
    return jax.shard_map(
        body, mesh=cut, in_specs=in_specs, out_specs=out_specs, check_vma=False
    )
```

```python
from functools import partial
import math

import jax
import jax.numpy as jnp
from jax import lax
from jax.experimental import pallas as pl
from jax.experimental.pallas import tpu as pltpu
from jax.sharding import Mesh, PartitionSpec as P

LAYERS = 2
EPS = 1e-05
HIGH = lax.Precision.HIGHEST
ROOT_TWO = math.sqrt(2.0)
ROOT_TWO_PI = math.sqrt(2.0 * math.pi)
F32 = jnp.float32
BF16 = jnp.bfloat16
LANES = 128
VMEM_LIMIT = 24 * 1024 * 1024
SMEM_SPEC = pl.BlockSpec(memory_space=pltpu.SMEM)
VMEM_SPEC = pl.BlockSpec(memory_space=pltpu.VMEM)


FLIP2 = [(0, 1), (1, 0)]
DIAGONAL = [(0, 3), (1, 2), (2, 1), (3, 0)]


def swap_half(array):
    return lax.ppermute(array, "l", FLIP2)


def after(value, *others):
    return lax.optimization_barrier((value, others))[0]


def split(value):
    high = value.astype(BF16)
    return high, (value - high.astype(F32)).astype(BF16)


def dot(a, b, dims):
    return lax.dot_general(a, b, (dims, ((), ())), preferred_element_type=F32)


NT = ((1,), (1,))
NN = ((1,), (0,))


def in_hbm(array):
    return pltpu.with_memory_space_constraint(array, pltpu.HBM)


def call(body, out_shape, hbm_outs=(), **kwargs):
    if hbm_outs:
        out_shape = [
            pltpu.HBM(a.shape, a.dtype) if i in hbm_outs else a for i, a in enumerate(out_shape)
        ]
    return pl.pallas_call(
        body,
        out_shape=out_shape,
        compiler_params=pltpu.CompilerParams(vmem_limit_bytes=VMEM_LIMIT),
        **kwargs,
    )


def cost(flops, byte_count):
    return pl.CostEstimate(flops=int(flops) // 64, bytes_accessed=int(byte_count) // 64, transcendentals=0)


def pack_body(frames, place_ref, in_ref, near_ref, far_ref, turned):
    slots = in_ref.shape[1]
    for start in range(0, slots, LANES):
        turned[start : start + LANES, :] = in_ref[:, start : start + LANES].T
    for rel in range(4):
        first = pl.multiple_of(place_ref[rel] * frames, 8)
        out = (near_ref, far_ref)[rel // 2]
        out[(rel % 2) * frames : (rel % 2 + 1) * frames, :] = turned[pl.ds(first, frames), :]


def pack(place, array, frames, waits=False):
    width, slots = array.shape
    out = jax.ShapeDtypeStruct((2 * frames, width), F32)
    return call(
        partial(pack_body, frames),
        grid=(1,),
        out_shape=[out, out],
        in_specs=[SMEM_SPEC, pl.BlockSpec((width, slots), lambda i: (0, 0))],
        out_specs=[pl.BlockSpec(out.shape, lambda i: (0, 0))] * 2,
        scratch_shapes=[pltpu.VMEM((slots, width), F32)],
        hbm_outs=(0, 1) if waits else (),
        cost_estimate=cost(0, 8 * width * slots),
        name="pack",
    )(place, in_hbm(array))


def part_spec(part, frames):
    array, i = part
    if i is None:
        return pl.BlockSpec(array.shape, lambda *_: (0,) * array.ndim)
    return pl.BlockSpec((frames, array.shape[1]), lambda *_: (i, 0))


def arrays_of(parts):
    return [array for array, _ in parts]


def unpack_body(frames, place_ref, *refs):
    ins, out_ref, turned = refs[:4], refs[4], refs[5]
    slots = out_ref.shape[1]
    for rel in range(4):
        first = pl.multiple_of(place_ref[rel] * frames, 8)
        turned[pl.ds(first, frames), :] = ins[rel][...]
    for start in range(0, slots, LANES):
        out_ref[:, start : start + LANES] = turned[start : start + LANES, :].T


def unpack(place, parts, frames, waited=False):
    width = parts[0][0].shape[1]
    slots = 4 * frames
    return call(
        partial(unpack_body, frames),
        grid=(1,),
        out_shape=jax.ShapeDtypeStruct((width, slots), F32),
        in_specs=[SMEM_SPEC] + [part_spec(part, frames) for part in parts],
        out_specs=pl.BlockSpec((width, slots), lambda i: (0, 0)),
        scratch_shapes=[pltpu.VMEM((slots, width), F32)],
        cost_estimate=cost(0, 8 * width * slots),
        name="unpack",
    )(place, *[in_hbm(a) if waited else a for a in arrays_of(parts)])


def merge_body(kept_ref, come_ref, out_ref):
    frames, columns = kept_ref.shape
    width = columns // 2
    for i in range(2):
        some = slice(i * width, (i + 1) * width)
        out_ref[i * frames : (i + 1) * frames, :] = kept_ref[:, some] + come_ref[:, some]


def merge(kept, half, come):
    frames, columns = come.shape
    return call(
        merge_body,
        grid=(1,),
        out_shape=jax.ShapeDtypeStruct((2 * frames, columns // 2), F32),
        in_specs=[
            pl.BlockSpec((frames, columns), lambda i: (0, half)),
            pl.BlockSpec((frames, columns), lambda i: (0, 0)),
        ],
        out_specs=pl.BlockSpec((2 * frames, columns // 2), lambda i: (0, 0)),
        cost_estimate=cost(0, 12 * frames * columns),
        name="merge",
    )(kept, come)


def project_body(n_parts, n_flat, spots, n_weights, first, with_acc, with_stats, with_params, cols_ref, place_ref, *refs):
    del cols_ref

    def take(n):
        nonlocal refs
        some, refs = refs[:n], refs[n:]
        return some

    parts, flat_parts, weights = take(n_parts), take(n_flat), take(n_weights)
    acc, valid, stats_in, params = take(with_acc), take(with_stats > 0), take(with_stats > 1), take(with_params)
    (out_ref,) = take(1)
    stats, flat = take(with_stats > 0), take(n_flat > 0)
    x_high, x_low, far_ref = refs
    step = pl.program_id(0)
    width = x_high.shape[2]

    @pl.when(step == 0)
    def _():
        for block, part in zip(spots, parts):
            for start in range(0, part.shape[1], width):
                high, low = split(part[:, start : start + width])
                x_high[block + start // width] = high
                x_low[block + start // width] = low
        column = 0
        for part in flat_parts:
            flat[0][:, column : column + part.shape[1]] = part[...]
            column += part.shape[1]
        if with_acc:
            out_ref[...] = acc[0][...]
        else:
            out_ref[...] = jnp.zeros_like(out_ref)

    stacked = jnp.concatenate([x_high[step], x_low[step], x_high[step]], axis=1)
    for block, weight in enumerate(weight_blocks(place_ref, weights, far_ref)):
        w_high, w_low = split(weight)
        columns = slice(block * width, (block + 1) * width)
        out_ref[:, columns] += dot(stacked, jnp.concatenate([w_high, w_high, w_low], axis=1), NT)

    if with_stats:
        (stats_ref,) = stats

        @pl.when(step == pl.num_programs(0) - 1)
        def _():
            if stats_in:
                stats_ref[...] = stats_in[0][...]
            own = jnp.sum(valid[0][...], axis=0, keepdims=True)
            per = width // LANES
            for row in range(out_ref.shape[1] // LANES):
                z = out_ref[:, row * LANES : (row + 1) * LANES]
                total = jnp.sum(valid[0][...] * z, axis=0, keepdims=True)
                centred = valid[0][...] * (z - total / own)
                squares = jnp.sum(centred * centred, axis=0, keepdims=True)
                at = place_ref[first + row // per] * per + row % per
                stats_ref[0, pl.ds(at, 1), :] = total
                stats_ref[1, pl.ds(at, 1), :] = squares
                stats_ref[2, pl.ds(at, 1), :] = own
            if with_params:
                rest = params[0].shape[0] - 8
                stats_ref[3] = params[0][:8, :]
                stats_ref[4] = jnp.zeros_like(stats_ref[4])
                stats_ref[4, :rest, :] = params[0][8:, :]


def weight_specs(weights, layer, pairs=2):
    specs = []
    for weight in weights:
        if weight.ndim == 3:
            shape = (1, weight.shape[1], pairs * weight.shape[1])
            specs.append(pl.BlockSpec(shape, lambda s, cols, *_: (layer, 0, cols[s])))
        else:
            shape = (weight.shape[0], pairs * 4 * weight.shape[0])
            specs.append(pl.BlockSpec(shape, lambda s, cols, *_: (0, cols[s])))
    return specs


def far_scratch(width, pairs=2):
    return pltpu.VMEM((2, width, pairs * width), F32)


def weight_blocks(place_ref, refs, far_ref):
    near = [ref[0] for ref in refs if len(ref.shape) == 3]
    pieces = [ref for ref in refs if len(ref.shape) == 2]
    far = []
    for i in range(len(pieces) // 4):
        for rel, piece in enumerate(pieces[4 * i : 4 * i + 4]):
            rows = piece.shape[0]
            row = 2 * (place_ref[4] ^ (rel // 2)) + (place_ref[5] ^ (rel % 2))
            far_ref[i, pl.ds(pl.multiple_of(row * rows, rows), rows), :] = piece[...]
        far.append(far_ref[i])
    return near + far


def project(
    place, frames, parts, blocks, weights, layer, acc=None, valid=None, stats=None, params=None, flat=()
):
    near = weights[0].ndim == 3
    units = sum(1 if w.ndim == 3 else 0.25 for w in weights)
    width = weights[0].shape[1] if near else 4 * weights[0].shape[0]
    n = blocks.shape[0]
    spots, block = [], 0
    for array, _ in parts:
        spots.append(block)
        block += array.shape[1] // width
    full = pl.BlockSpec(memory_space=pltpu.VMEM)
    in_specs = [part_spec(part, frames) for part in (*parts, *flat)]
    in_specs += weight_specs(weights, layer, 1)
    operands = arrays_of(parts) + arrays_of(flat) + [in_hbm(w) for w in weights]
    array = jax.ShapeDtypeStruct((frames, int(units) * width), F32)
    array_spec = pl.BlockSpec(array.shape, lambda s, cols, place: (0, 0))
    out_shape, out_specs = [array], [array_spec]
    if acc is not None:
        in_specs.append(array_spec)
        operands.append(in_hbm(acc))
    if valid is not None:
        in_specs.append(full)
        operands.append(valid)
        shape = (3 if params is None else 5, 4 * width // LANES, LANES)
        out_shape.append(jax.ShapeDtypeStruct(shape, F32))
        out_specs.append(pl.BlockSpec(shape, lambda s, cols, place: (0, 0, 0)))
    for extra in (stats, params):
        if extra is not None:
            in_specs.append(full)
            operands.append(extra)
    if flat:
        out_shape.append(jax.ShapeDtypeStruct((frames, 4 * width), F32))
        out_specs.append(pl.BlockSpec((frames, 4 * width), lambda s, cols, place: (0, 0)))
    return call(
        partial(
            project_body,
            len(parts),
            len(flat),
            spots,
            len(weights),
            0 if near else 2,
            acc is not None,
            (valid is not None) + (stats is not None),
            params is not None,
        ),
        grid_spec=pltpu.PrefetchScalarGridSpec(
            num_scalar_prefetch=2,
            grid=(n,),
            in_specs=in_specs,
            out_specs=out_specs,
            scratch_shapes=[pltpu.VMEM((n, frames, width), BF16)] * 2 + [far_scratch(width, 1)],
        ),
        out_shape=out_shape,
        hbm_outs=(0, len(out_shape) - 1) if flat else (0,),
        cost_estimate=cost(6 * frames * n * width * units * width, 4 * n * width * units * width),
        name="project",
    )(blocks, place, *operands)


def to_relative(place_ref, spread, rows_ref, value, slot):
    per = value.shape[0] // 4
    spread[...] = value
    for rel in range(4):
        first = place_ref[rel] * per
        for row in range(per):
            rows_ref[slot, rel * per + row : rel * per + row + 1, :] = spread[
                pl.ds(first + row, 1), :
            ]


def tree(values):
    while len(values) > 1:
        values = [a + b for a, b in zip(values[::2], values[1::2])]
    return values[0]


def gathered(ref, slot):
    return [ref[i] for i in range(slot, ref.shape[0], ref.shape[0] // 16)]


def norm_terms(stats_ref):
    each = [gathered(stats_ref, slot) for slot in range(3)]
    totals, squares, owns = each
    count = tree(owns)
    mean = tree(totals) / count
    away = [total / own - mean for total, own in zip(totals, owns)]
    spread = tree([s + n * a * a for s, n, a in zip(squares, owns, away)])
    return count, mean, lax.rsqrt(spread / count + EPS)


CHUNKS = 4


def columns_of(refs, row):
    for ref in refs:
        if row * LANES < ref.shape[1]:
            return ref[:, row * LANES : (row + 1) * LANES]
        row -= ref.shape[1] // LANES


def recur_body(n_z, last, layer, spread_params, place_ref, gate_ref, *refs):
    z_refs, refs = refs[:n_z], refs[n_z:]
    (stats_ref, params_ref, valid_ref, x_ref), refs = refs[:4], refs[4:]
    outs, refs = refs[: 1 + 3 * last], refs[1 + 3 * last :]
    if spread_params:
        state_ref, slope_ref, params_out, rows, spread, held, drive_s, state_s, slope_s = refs
    else:
        state_ref, slope_ref, rows, spread, held, drive_s, state_s, slope_s = refs
    frames, features = x_ref.shape
    blocks = features // LANES
    per = blocks // 4
    chunk = pl.program_id(0)

    @pl.when(chunk == 0)
    def _():
        if spread_params:
            for rel in range(4):
                first = place_ref[rel] * (stats_ref.shape[0] // 16) + 3
                for row in range(LAYERS * 3 * per):
                    at = rel * per + row % per
                    params_out[row // per, at : at + 1, :] = stats_ref[
                        first + row // 8, row % 8 : row % 8 + 1, :
                    ]
            params = [params_out[3 * layer + i] for i in range(3)]
        else:
            params = [params_ref[3 * layer + i] for i in range(3)]
        _, mean, inv_std = norm_terms(stats_ref)
        to_relative(place_ref, spread, rows, mean, 0)
        to_relative(place_ref, spread, rows, inv_std, 1)
        rows[1] = rows[1] * params[0]
        rows[2] = params[1]
        rows[3] = params[2]
        held[...] = jnp.zeros_like(held)

    for row in range(blocks):
        drive_s[row * frames : (row + 1) * frames, :] = (
            columns_of(z_refs, row) - rows[0, row : row + 1, :]
        ) * rows[1, row : row + 1, :] + rows[2, row : row + 1, :]
    decay = rows[3]

    def step(t, state):
        at = pl.ds(t, blocks, stride=frames)
        pre = drive_s[at, :] + decay * state
        half = 0.5 + 0.5 * lax.erf(pre * (1.0 / ROOT_TWO))
        gate = gate_ref[chunk * frames + t] > 0.0
        slope = half + pre * jnp.exp(-0.5 * pre * pre) * (1.0 / ROOT_TWO_PI)
        state = jnp.where(gate, pre * half, state)
        state_s[at, :] = state
        slope_s[at, :] = jnp.where(gate, slope, 0.0)
        return state

    held[...] = lax.fori_loop(0, frames, step, held[...], unroll=8)
    valid = valid_ref[...]
    for row in range(blocks):
        lanes = slice(row * LANES, (row + 1) * LANES)
        state = state_s[row * frames : (row + 1) * frames, :]
        state_ref[:, lanes] = state
        slope_ref[:, lanes] = slope_s[row * frames : (row + 1) * frames, :]
        value = x_ref[:, lanes] + valid * state
        out, at = (outs[row // per], row % per) if last else (outs[0], row)
        out[:, at * LANES : (at + 1) * LANES] = value


def recur(layer, place, gate, z, stats, params, valid, x, last):
    frames, features = x.shape
    blocks = features // LANES
    some = frames // CHUNKS
    whole = lambda array: pl.BlockSpec(array.shape, lambda i: (0,) * array.ndim)
    by_chunk = lambda array: pl.BlockSpec((some, array.shape[1]), lambda i: (i, 0))
    full = jax.ShapeDtypeStruct((frames, features), F32)
    piece = jax.ShapeDtypeStruct((frames, features // 4), F32)
    out_shape = [piece] * 4 if last else [full]
    out_shape += [full, full]
    out_specs = [by_chunk(a) for a in out_shape]
    spread_params = params is None
    if spread_params:
        out_shape.append(jax.ShapeDtypeStruct((3 * LAYERS, blocks, LANES), F32))
        out_specs.append(whole(out_shape[-1]))
        params = valid
    return call(
        partial(recur_body, len(z), last, layer, spread_params),
        grid=(CHUNKS,),
        in_specs=[SMEM_SPEC, SMEM_SPEC]
        + [by_chunk(a) for a in z]
        + [whole(a) for a in (stats, params)]
        + [by_chunk(a) for a in (valid, x)],
        out_specs=out_specs,
        out_shape=out_shape,
        hbm_outs=tuple(range(len(out_shape) - spread_params)) if last else (1, 2),
        scratch_shapes=[
            pltpu.VMEM((4, blocks, LANES), F32),
            pltpu.VMEM((blocks, LANES), F32),
            pltpu.VMEM((blocks, LANES), F32),
        ]
        + [pltpu.VMEM((blocks * some, LANES), F32)] * 3,
        cost_estimate=cost(100 * frames * features, 20 * frames * features),
        name="recur",
    )(place, gate, *[in_hbm(a) for a in z], stats, params, valid, in_hbm(x))


def back_body(n_z, n_ups, spots, layer, place_ref, gate_ref, *refs):
    z_refs, refs = refs[:n_z], refs[n_z:]
    (stats_ref, params_ref), refs = refs[:2], refs[2:]
    ups, (state_ref, slope_ref), refs = refs[:n_ups], refs[n_ups : n_ups + 2], refs[n_ups + 2 :]
    grad_ref, sums_ref, rows, spread, held, up_s, state_s, slope_s = refs
    frames, features = state_ref.shape
    blocks = features // LANES
    per = blocks // 4
    tall = frames + 8
    step_no = pl.program_id(0)
    chunk = pl.num_programs(0) - 1 - step_no

    @pl.when(step_no == 0)
    def _():
        _, mean, inv_std = norm_terms(stats_ref)
        to_relative(place_ref, spread, rows, mean, 0)
        to_relative(place_ref, spread, rows, inv_std, 1)
        held[...] = jnp.zeros_like(held)

    for row in range(blocks):
        lanes = slice(row * LANES, (row + 1) * LANES)
        base = row * frames
        up = None
        for (_, column), part in zip(spots, ups):
            if column <= row * LANES < column + part.shape[1]:
                value = part[:, row * LANES - column : (row + 1) * LANES - column]
                up = value if up is None else up + value
        up_s[base : base + frames, :] = up
        state_s[row * tall : row * tall + 8, :] = jnp.zeros((8, LANES), F32)
        state_s[row * tall + 8 : (row + 1) * tall, :] = state_ref[:, lanes]
        slope_s[base : base + frames, :] = slope_ref[:, lanes]
    decay = params_ref[3 * layer + 2]

    def step(i, carry):
        t = frames - 1 - i
        at = pl.ds(t, blocks, stride=frames)
        slope = slope_s[at, :]
        gate = gate_ref[chunk * frames + t]
        total = gate * up_s[at, :] + carry
        up_s[at, :] = total * slope
        return total * (slope * decay + (1.0 - gate))

    held[0] = lax.fori_loop(0, frames, step, held[0], unroll=8)
    held[4] += held[1] * state_s[pl.ds(tall - 1, blocks, stride=tall), :]
    held[1] = up_s[pl.ds(0, blocks, stride=frames), :]
    for row in range(blocks):
        lanes = slice(row * LANES, (row + 1) * LANES)
        grad = up_s[row * frames : (row + 1) * frames, :]
        grad_ref[:, lanes] = grad
        zhat = (columns_of(z_refs, row) - rows[0, row : row + 1, :]) * rows[1, row : row + 1, :]
        before = state_s[row * tall + 7 : row * tall + 7 + frames, :]
        for slot, value in enumerate((grad * zhat, grad, grad * before)):
            held[2 + slot, row : row + 1, :] += jnp.sum(value, axis=0, keepdims=True)

    @pl.when(chunk == 0)
    def _():
        for row in range(blocks):
            at = place_ref[row // per] * per + row % per
            for slot in range(3):
                sums_ref[slot, pl.ds(at, 1), :] = held[2 + slot, row : row + 1, :]


def spots_of_sum(parts, width):
    spots, column = [], 0
    for array, _ in parts:
        spots.append((0, column % (4 * width)))
        column += array.shape[1]
    return spots


def back(layer, place, gate, z, stats, params, ups, states, slopes):
    frames, features = states.shape
    width = features // 4
    blocks = features // LANES
    some = frames // CHUNKS
    whole = lambda array: pl.BlockSpec(array.shape, lambda i: (0,) * array.ndim)

    def by_chunk(array, first=0):
        return pl.BlockSpec(
            (some, array.shape[1]), lambda i: ((first or 0) * CHUNKS + CHUNKS - 1 - i, 0)
        )

    out_shape = [
        jax.ShapeDtypeStruct((frames, features), F32),
        jax.ShapeDtypeStruct((3, blocks, LANES), F32),
    ]
    return call(
        partial(back_body, len(z), len(ups), spots_of_sum(ups, width), layer),
        grid=(CHUNKS,),
        in_specs=[SMEM_SPEC] * 2
        + [by_chunk(a) for a in z]
        + [whole(a) for a in (stats, params)]
        + [by_chunk(*up) for up in ups]
        + [by_chunk(a) for a in (states, slopes)],
        out_specs=[by_chunk(out_shape[0]), whole(out_shape[1])],
        out_shape=out_shape,
        scratch_shapes=[
            pltpu.VMEM((2, blocks, LANES), F32),
            pltpu.VMEM((blocks, LANES), F32),
            pltpu.VMEM((5, blocks, LANES), F32),
            pltpu.VMEM((blocks * some, LANES), F32),
            pltpu.VMEM((blocks * (some + 8), LANES), F32),
            pltpu.VMEM((blocks * some, LANES), F32),
        ],
        cost_estimate=cost(30 * frames * features, 20 * frames * features),
        name="back",
    )(
        place,
        gate,
        *[in_hbm(a) for a in z],
        stats,
        params,
        *arrays_of(ups),
        in_hbm(states),
        in_hbm(slopes),
    )


def input_terms(high_s, low_s, weights):
    left, right = [], []
    for block, weight in enumerate(weights):
        w_high, w_low = split(weight)
        left += [high_s[block], low_s[block], high_s[block]]
        right += [w_high, w_high, w_low]
    return dot(jnp.concatenate(left, axis=1), jnp.concatenate(right, axis=0), NN)


def norm_back_body(n_z, split_terms, layer, cols_ref, place_ref, grad_ref, *refs):
    del cols_ref
    z_refs, refs = refs[:n_z], refs[n_z:]
    params_ref, valid_ref, stats_ref, sums_ref, *refs = refs
    weights, refs = refs[:10], refs[10:]
    if split_terms:
        out_ref, leave_ref, near_term_ref, far_term_ref, sums_out_ref, *refs = refs
        term_refs, starts = (far_term_ref, near_term_ref), (0, 0)
    else:
        out_ref, leave_ref, term_ref, sums_out_ref, *refs = refs
        term_refs, starts = (term_ref, term_ref), (2 * grad_ref.shape[1] // 4, 0)
    rows, spread, high_s, low_s, far_ref = refs
    blocks = grad_ref.shape[1] // LANES
    width = high_s.shape[2]
    per = width // LANES

    @pl.when(pl.program_id(0) == 0)
    def _():
        count, mean, inv_std = norm_terms(stats_ref)
        to_relative(place_ref, spread, rows, mean, 0)
        to_relative(place_ref, spread, rows, inv_std, 1)
        rows[2] = rows[1] * params_ref[3 * layer]
        sums = [tree(gathered(sums_ref, slot)) for slot in range(3)]
        for slot in range(3):
            sums_out_ref[slot] = sums[slot]
        to_relative(place_ref, spread, rows, sums[0] / count, 3)
        to_relative(place_ref, spread, rows, sums[1] / count, 4)
        valid = valid_ref[...]
        for row in range(blocks):
            lanes = slice(row * LANES, (row + 1) * LANES)
            one = lambda slot: rows[slot, row : row + 1, :]
            zhat = (columns_of(z_refs, row) - one(0)) * one(1)
            value = one(2) * (grad_ref[:, lanes] - valid * (one(4) + zhat * one(3)))
            out_ref[:, lanes] = value
            if (row // per) % 2:
                at = (row // per // 2) * width + (row % per) * LANES
                leave_ref[:, at : at + LANES] = value
            high, low = split(value)
            inner = slice((row % per) * LANES, (row % per + 1) * LANES)
            high_s[row // per, :, inner] = high
            low_s[row // per, :, inner] = low

    value = input_terms(high_s, low_s, weight_blocks(place_ref, weights, far_ref))
    for step, (term_ref, first) in enumerate(zip(term_refs, starts)):

        @pl.when(pl.program_id(0) == step)
        def _():
            for pair in range(2):
                at = pl.multiple_of(((place_ref[0] & 1) ^ pair) * width, width)
                term_ref[:, pl.ds(first + at, width)] = value[
                    :, pair * width : (pair + 1) * width
                ]


def norm_back(columns, place, grad, z, params, valid, stats, sums, weights, layer, split_terms):
    frames, features = grad.shape
    width = features // 4
    blocks = features // LANES
    whole = lambda array: pl.BlockSpec(array.shape, lambda s, cols, place: (0,) * array.ndim)
    operands = [grad, *[in_hbm(a) for a in z], params, valid, stats, sums]
    full = jax.ShapeDtypeStruct((frames, features), F32)
    half = jax.ShapeDtypeStruct((frames, 2 * width), F32)
    terms = [half, half] if split_terms else [full]
    out_shape = [full, half, *terms, jax.ShapeDtypeStruct((3, blocks, LANES), F32)]
    return call(
        partial(norm_back_body, len(z), split_terms, layer),
        grid_spec=pltpu.PrefetchScalarGridSpec(
            num_scalar_prefetch=2,
            grid=(2,),
            in_specs=[whole(a) for a in operands] + weight_specs(weights, layer),
            out_specs=[whole(a) for a in out_shape],
            scratch_shapes=[
                pltpu.VMEM((5, blocks, LANES), F32),
                pltpu.VMEM((blocks, LANES), F32),
                pltpu.VMEM((4, frames, width), BF16),
                pltpu.VMEM((4, frames, width), BF16),
                far_scratch(width),
            ],
        ),
        out_shape=out_shape,
        hbm_outs=(0,),
        cost_estimate=cost(6 * frames * features * features, 4 * features * features),
        name="norm_back",
    )(columns, place, *operands, *[in_hbm(w) for w in weights])


def own_terms_body(n_ups, spots, cols_ref, place_ref, grad_ref, *refs):
    del cols_ref
    ups, refs = refs[:n_ups], refs[n_ups:]
    weights, refs = refs[:10], refs[10:]
    out_ref, high_s, low_s, far_ref = refs
    width = high_s.shape[2]
    step = pl.program_id(0)

    @pl.when(step == 0)
    def _():
        for block in range(4):
            high, low = split(grad_ref[:, block * width : (block + 1) * width])
            high_s[block] = high
            low_s[block] = low

    value = input_terms(high_s, low_s, weight_blocks(place_ref, weights, far_ref))
    for pair in range(2):
        at = pl.multiple_of(((place_ref[0] & 1) ^ pair) * width, width)
        out_ref[:, pl.ds(at, width)] = value[:, pair * width : (pair + 1) * width]
    for half in range(2):

        @pl.when(step == half)
        def _():
            first = 2 * half * width
            for (_, column), up in zip(spots, ups):
                low = max(column, first)
                high = min(column + up.shape[1], first + 2 * width)
                if low < high:
                    out_ref[:, low - first : high - first] += up[:, low - column : high - column]


def own_terms(columns, place, grad, ups, weights, layer):
    frames, features = grad.shape
    width = features // 4
    whole = lambda array: pl.BlockSpec(array.shape, lambda s, cols, place: (0,) * array.ndim)
    step_block = pl.BlockSpec((frames, 2 * width), lambda s, cols, place: (0, s))
    return call(
        partial(own_terms_body, len(ups), spots_of_sum(ups, width)),
        grid_spec=pltpu.PrefetchScalarGridSpec(
            num_scalar_prefetch=2,
            grid=(2,),
            in_specs=[whole(grad)]
            + [part_spec(up, frames) for up in ups]
            + weight_specs(weights, layer),
            out_specs=step_block,
            scratch_shapes=[pltpu.VMEM((4, frames, width), BF16)] * 2 + [far_scratch(width)],
        ),
        out_shape=jax.ShapeDtypeStruct((frames, features), F32),
        cost_estimate=cost(6 * frames * features * features, 4 * features * features),
        name="own_terms",
    )(columns, place, in_hbm(grad), *arrays_of(ups), *[in_hbm(w) for w in weights])


def prepare_body(lists_ref, place_ref, own_ref, near_ref, high_ref, low_ref):
    del lists_ref
    padded = high_ref.shape[0] // 2
    width = high_ref.shape[1] // 2
    for clip, part in enumerate((own_ref, near_ref)):
        rows = part.shape[0]
        for dc in range(2):
            at = pl.multiple_of((place_ref[6] ^ clip ^ dc) * width, width)
            high, low = split(part[:, dc * width : (dc + 1) * width])
            high_ref[clip * padded : clip * padded + rows, pl.ds(at, width)] = high
            low_ref[clip * padded : clip * padded + rows, pl.ds(at, width)] = low
        zeros = jnp.zeros((padded - rows, 2 * width), BF16)
        high_ref[clip * padded + rows : (clip + 1) * padded, :] = zeros
        low_ref[clip * padded + rows : (clip + 1) * padded, :] = zeros


def prepare(place, own, near):
    frames, features = own.shape
    width = features // 4
    padded = -(-frames // LANES) * LANES
    in_spec = pl.BlockSpec((frames, 2 * width), lambda s, *_: (0, s))
    out = jax.ShapeDtypeStruct((2 * padded, features), BF16)
    out_spec = pl.BlockSpec((2 * padded, 2 * width), lambda s, order, place: (0, order[s]))
    order = jnp.stack([place[0] >> 1, 1 - (place[0] >> 1)])
    return call(
        prepare_body,
        grid_spec=pltpu.PrefetchScalarGridSpec(
            num_scalar_prefetch=2,
            grid=(2,),
            in_specs=[in_spec, in_spec],
            out_specs=[out_spec, out_spec],
        ),
        out_shape=[out, out],
        hbm_outs=(0, 1),
        cost_estimate=cost(0, 16 * frames * features),
        name="prepare",
    )(order, place, in_hbm(own), in_hbm(near))


def product(g_high, g_low, x_high, x_low):
    return dot(g_high, x_high, NN) + (dot(g_high, x_low, NN) + dot(g_low, x_high, NN))


def weight_body(turn, place_ref, *refs):
    if turn:
        grad_ref, near_ref, x_high, x_low, kept, sent, g_high, g_low, t_high, t_low = refs

        @pl.when(pl.program_id(0) == 0)
        def _():
            frames, features = grad_ref.shape
            width = features // 4
            rows = width // 4
            padded = t_high.shape[1] // 2
            t_high[...] = jnp.zeros_like(t_high)
            t_low[...] = jnp.zeros_like(t_low)
            for clip in range(2):
                for dh in range(2):
                    if clip == 0:
                        part = grad_ref[:, 2 * dh * width : (2 * dh + 1) * width]
                    else:
                        part = near_ref[:, dh * width : (dh + 1) * width]
                    high, low = split(part.T)
                    at = (
                        slice(dh * width, (dh + 1) * width),
                        slice(clip * padded, clip * padded + frames),
                    )
                    t_high[at] = high
                    t_low[at] = low
            for group in range(8):
                first, second, dh = group // 4, group // 2 % 2, group % 2
                core = place_ref[6]
                y = place_ref[4] ^ (first * core + second * (1 - core))
                x = place_ref[5] ^ (first * (1 - core) + second * core)
                at = pl.multiple_of(dh * width + (2 * y + x) * rows, rows)
                g_high[group * rows : (group + 1) * rows, :] = t_high[pl.ds(at, rows), :]
                g_low[group * rows : (group + 1) * rows, :] = t_low[pl.ds(at, rows), :]

    else:
        g_high, g_low, x_high, x_low, kept, sent = refs
    half = g_high.shape[0] // 2
    value = product(g_high[...], g_low[...], x_high[...], x_low[...])
    kept[...] = value[:half].reshape(kept.shape)
    sent[...] = value[half:].reshape(sent.shape)


def weight_rows(side, place, grads, x_split, width):
    turn = side == 0
    whole = lambda array: pl.BlockSpec(array.shape, lambda s, place: (0,) * array.ndim)
    x_spec = pl.BlockSpec((x_split[0].shape[0], width), lambda s, place: (0, s))
    shape = (2, 2, width // 4, 4 * width)
    out_shape = [jax.ShapeDtypeStruct(shape, F32)] * 2
    out_specs = [pl.BlockSpec(shape[:3] + (width,), lambda s, place: (0, 0, 0, s))] * 2
    scratch = []
    if turn:
        turned = (2 * width, x_split[0].shape[0])
        out_shape += [jax.ShapeDtypeStruct(turned, BF16)] * 2
        out_specs += [whole(out_shape[-1])] * 2
        scratch = [pltpu.VMEM(turned, BF16)] * 2
    return call(
        partial(weight_body, turn),
        grid_spec=pltpu.PrefetchScalarGridSpec(
            num_scalar_prefetch=1,
            grid=(4,),
            in_specs=[whole(a) for a in grads] + [x_spec] * 2,
            out_specs=out_specs,
            scratch_shapes=scratch,
        ),
        out_shape=out_shape,
        hbm_outs=(0,),
        cost_estimate=cost(12 * x_split[0].shape[0] * width * 4 * width, 4 * 8 * width * width),
        name="weight_rows",
    )(place, *([in_hbm(grads[0]), grads[1]] if turn else grads), *[in_hbm(x) for x in x_split])


def step_body(n, widths, cut, *refs):
    ins, outs = refs[: 2 * n], refs[2 * n :]
    starts = [sum(widths[:i]) for i in range(len(widths))]
    column = 0
    for i in range(n):
        total = ins[2 * i][...] + ins[2 * i + 1][...]
        end = column + total.shape[-1]
        for j, (start, columns) in enumerate(zip(starts, widths)):
            low, high = max(start, column), min(start + columns, end)
            if low < high:
                to = (Ellipsis, slice(low - start, high - start))
                piece = total[..., low - column : high - column]
                if cut:
                    outs[2 * j][to] = piece[0]
                    outs[2 * j + 1][to] = piece[1]
                else:
                    outs[j][to] = piece
        column = end


def step_of(*pairs, cut=True, widths=None):
    shape = list(pairs[0][0].shape)
    widths = widths or [sum(pair[0].shape[-1] for pair in pairs)]
    outs = []
    for columns in widths:
        shape[-1] = columns
        out = jax.ShapeDtypeStruct(tuple(shape[1:] if cut else shape), F32)
        outs += [out] * (1 + cut)
    whole = lambda array: pl.BlockSpec(array.shape, lambda i: (0,) * array.ndim)
    operands = [array for pair in pairs for array in pair]
    return call(
        partial(step_body, len(pairs), widths, cut),
        grid=(1,),
        in_specs=[whole(a) for a in operands],
        out_specs=[whole(a) for a in outs],
        out_shape=outs,
        cost_estimate=cost(0, 4 * sum(a.size for a in operands)),
        name="reduction_step",
    )(*operands)


def plane_swap(array, step):
    pairs = []
    for i in range(8):
        over_x = (i % 2 == 0) == (step == 0)
        pairs.append((i, i ^ 2 if over_x else i ^ 4))
    return lax.ppermute(array, ("y", "x", "c"), pairs)


def plane_gather(share, *before):
    first = plane_swap(share, 0)
    second = plane_swap(share, 1)
    return [share, second, first, plane_swap(after(first, *before), 1)]


def assemble_body(by_core, place_ref, *refs):
    out_ref = refs[-1]
    core = place_ref[6] if by_core else 1
    rows, columns = refs[0].shape
    quarter = columns // 4
    for i in range(4):
        first, second = i // 2, i % 2
        y = place_ref[4] ^ (first * core + second * (1 - core))
        x = place_ref[5] ^ (first * (1 - core) + second * core)
        at = pl.multiple_of((2 * y + x) * rows, rows)
        for side in range(2):
            for h in range(2):
                to = pl.multiple_of((2 * h + (place_ref[7] ^ side)) * quarter, quarter)
                some = slice((2 * side + h) * quarter, (2 * side + h + 1) * quarter)
                out_ref[0, pl.ds(at, rows), pl.ds(to, quarter)] = refs[i][:, some]


def assemble(place, pieces, layer, onto=None, by_core=True):
    rows, columns = 4 * pieces[0].shape[0], pieces[0].shape[1]
    aliases, extra, extra_specs = {}, [], []
    if onto is not None:
        aliases, extra = {1 + len(pieces): 0}, [onto]
        extra_specs = [pl.BlockSpec(memory_space=pl.ANY)]
    (out,) = call(
        partial(assemble_body, by_core),
        grid=(1,),
        out_shape=[jax.ShapeDtypeStruct((LAYERS, rows, columns), F32)],
        hbm_outs=(0,),
        in_specs=[SMEM_SPEC]
        + [pl.BlockSpec(p.shape, lambda i: (0, 0)) for p in pieces]
        + extra_specs,
        out_specs=[pl.BlockSpec((1, rows, columns), lambda i: (layer, 0, 0))],
        input_output_aliases=aliases,
        cost_estimate=cost(0, 8 * rows * columns),
        name="assemble",
    )(place, *[p if extra else in_hbm(p) for p in pieces], *extra)
    return out


def half_features(inputs, weights, gains, shifts, decays, biases, lengths, frame_mask, grad_out):
    width, slots = inputs.shape
    clips, frames = frame_mask.shape
    depth = weights.shape[2]
    blocks = 4 * width // LANES
    y, x, h, l, c = (lax.axis_index(name) for name in ("y", "x", "h", "l", "c"))
    b = 2 * y + x
    numbers = [2 * (h ^ (rel // 2)) + (c ^ (rel % 2)) for rel in range(4)] + [y, x, c, l]
    place = jnp.stack(numbers).astype(jnp.int32)
    own_blocks, other_blocks = (
        jnp.stack(
            [2 * (2 * (h ^ (rel // 2)) + half) + (c ^ (rel % 2)) for rel in range(4)]
        ).astype(jnp.int32)
        for half in (l, 1 - l)
    )
    own_columns = jnp.stack([2 * h + l, 2 * (1 - h) + l]).astype(jnp.int32)
    other_columns = jnp.stack([2 * (1 - h) + 1 - l, 2 * h + 1 - l]).astype(jnp.int32)
    rows = width // 4

    clip = 2 * h + c
    seen = lax.dynamic_index_in_dim(frame_mask, clip, 0, keepdims=False)
    length = lax.dynamic_index_in_dim(lengths, clip, 0, keepdims=False)
    moments = jnp.arange(frames, dtype=jnp.int32)
    gate = ((moments < length) & ((seen == 1) | (moments == 0))).astype(F32)
    valid = jnp.broadcast_to(gate[:, None], (frames, LANES))

    def far_share(layer):
        return lax.dynamic_slice(weights, (layer, b * rows, 0), (1, rows, depth))[0]

    def over_h(array):
        return lax.ppermute(array, "h", FLIP2)

    def over_c(array):
        return lax.ppermute(array, "c", FLIP2)

    def over_second(array):
        return plane_swap(array, 1)

    def four_of(near_rows, far_rows):
        return [
            (near_rows, 0),
            (over_c(near_rows), 1),
            (far_rows, 0),
            (over_c(far_rows), 1),
        ]

    def four_of_plane(share):
        both = lax.ppermute(share, ("y", "x"), DIAGONAL)
        return [share, lax.ppermute(share, "x", FLIP2), lax.ppermute(share, "y", FLIP2), both]

    near = over_c(weights)
    share = far_share(0)
    close, away = pack(place, after(inputs, share), frames)
    share = over_h(share)
    away = over_h(away)
    other_close = swap_half(close)
    up_close, up_away = pack(place, after(grad_out, close), frames, waits=True)
    share = after(share, up_close, valid, near, other_close)
    pieces = four_of_plane(share)
    away = after(away, pieces[1:])
    half_weights = [[weights, near, *pieces, *map(over_c, after(pieces, away))]]
    own = four_of(after(close, away), away)
    other_away = swap_half(away)
    others = [(other_close, 0), (over_c(other_close), 1)]
    params = jnp.stack([gains, shifts + biases, decays], axis=1)
    own_params = params.reshape(LAYERS * 3 * width // LANES, LANES)
    params = None

    def gather(array, axes):
        return lax.all_gather(array, axes, tiled=True)

    weight = half_weights[0]
    early = jnp.concatenate([own_blocks, other_blocks[:2]])
    z, own_flat = project(place, frames, own + others, early, weight, 0, flat=own)
    others += [(other_away, 0), (over_c(after(other_away, z)), 1)]
    z, stats, other_flat = project(
        place,
        frames,
        others[2:],
        other_blocks[2:],
        weight,
        0,
        z,
        valid,
        params=own_params,
        flat=others,
    )
    z = [z]
    stats = gather(stats, ("h", "c"))
    share = over_c(lax.ppermute(after(far_share(1), stats), ("h", "c"), DIAGONAL))
    stats = gather(stats, ("y", "x"))
    x, states, slopes, params = recur(0, place, gate, z, stats, None, valid, own_flat, False)
    own_near, other_near = over_c(after(own_flat, z[0])), over_c(after(other_flat, z[0]))
    x_near = over_c(x)
    own_split = prepare(place, after(own_flat, x_near), own_near)
    other_split = prepare(place, after(other_flat, x_near), other_near)
    saved = [(own_split, other_split, z, stats, states, slopes)]

    pieces = four_of_plane(after(share, slopes, own_near, other_near))
    near = [weights, near]
    other = swap_half(x)
    x_own = after(x, own_split[0], other_split[0])
    z, *_ = project(place, frames, [(x_own, None)], own_blocks, near, 1)
    own_split = prepare(place, after(x, z), x_near)
    far = [*pieces, *map(over_c, after(pieces, own_split[0]))]
    up_away = over_h(after(up_away, other, own_split[0]))
    half_weights.append(near + far)
    z, stats = project(place, frames, [(other, None)], other_blocks, near, 1, z, valid)
    both = jnp.concatenate([own_blocks, other_blocks])
    z_far, stats = project(
        place,
        frames,
        [(x, None), (other, None)],
        both,
        far,
        1,
        None,
        valid,
        stats,
    )
    z = [z, z_far]
    stats = gather(gather(stats, ("y", "x")), ("h", "c"))
    upstream = four_of(up_close, after(up_away, stats))
    *output, states, slopes = recur(1, place, gate, z, stats, params, valid, x, True)
    other_near = over_c(after(other, slopes))
    saved.append((own_split, (other, other_near), z, stats, states, slopes))
    diagonal = over_c(over_h(output[3]))

    ups = upstream
    results = [None] * LAYERS
    for layer in range(LAYERS - 1, -1, -1):
        own_split, other_split, z, stats, states, slopes = saved[layer]
        weight = half_weights[layer]
        grad_pre, sums = back(layer, place, gate, z, stats, params, ups, states, slopes)
        sums = gather(sums, ("y", "x"))
        if layer == 0:
            come[0] = after(come[0], sums)
            later, go = step_of((in_hbm(stay[0]), come[0]), (in_hbm(stay[1]), come[1]))
            sums = after(sums, later)
            go = over_second(go)
        sums = gather(sums, ("h", "c"))
        if layer > 0:
            away = over_h(after(output[2], sums))
        grad_z, leaving, *terms, sums = norm_back(
            other_columns, place, grad_pre, z, params, valid, stats, sums, weight, layer,
            layer == 0,
        )
        leaving = over_c(leaving)
        if layer > 0:
            received = [swap_half(terms[0])]
            other_split = prepare(place, *after(other_split, grad_z))
            leaving = after(leaving, diagonal, other_split[0])
        else:
            received = [None, swap_half(terms[1])]
            later, go = step_of((later, after(go, grad_z)))
            leaving = after(leaving, later)
            go = lax.ppermute(go, ("h", "c"), DIAGONAL)
            later = (later, go)
        *first, g_high, g_low = weight_rows(0, place, (grad_z, leaving), own_split, width)
        turned = (g_high, g_low)
        come = [plane_swap(first[1], 0)]
        if layer > 0:
            turned = after(turned, away)
            output = [(a, 0) for a in (output[0], over_c(output[1]), away, diagonal)]
        else:
            received[0] = swap_half(after(terms[0], received[1]))
        second = weight_rows(1, place, turned, other_split, width)
        come.append(plane_swap(second[1], 0))
        stay = (first[0], second[0])
        kept = own_terms(own_columns, place, after(grad_z, second[0]), ups, weight, layer)
        ups = [(kept, None)] + [(r, None) for r in received]
        results[layer] = lax.dynamic_index_in_dim(
            sums.reshape(3, 4, width), clip, axis=1, keepdims=False
        )

    sums = jnp.stack(results)
    sums = [sums[:, 0], sums[:, 1], sums[:, 2]]
    away = merge(kept, 1, received[1])
    later = (later[0], over_c(after(later[1], away)))
    come[0] = after(come[0], sums, later[1])
    far = lax.ppermute(away, ("h", "c"), DIAGONAL)
    away = over_c(far)
    total, go = step_of((in_hbm(stay[0]), come[0]), (in_hbm(stay[1]), come[1]))
    go = over_second(go)
    (later,) = step_of(later, cut=False)
    later = four_of_plane(later)
    total, go = step_of((total, after(go, away)))
    go = over_h(go)
    output = unpack(place, [(after(array, total), i) for array, i in output], frames, waited=True)
    close = merge(kept, 0, after(received[0], output))
    grad_in = [(close, 0), (over_c(close[frames:]), 0), (away, 0), (far, 1)]
    grad_in = unpack(place, grad_in, frames)
    grad_weights = assemble(place, after(later, grad_in), 1, by_core=False)
    (share,) = step_of((total, after(go, grad_weights)), cut=False)
    gathered = plane_gather(share)
    grad_weights = assemble(place, gathered, 0, grad_weights)
    return (output, grad_in, grad_weights, *sums, sums[1])


def gelu_slope(value):
    return (
        0.5 * (1.0 + jax.scipy.special.erf(value / ROOT_TWO))
        + value * jnp.exp(-0.5 * value * value) / ROOT_TWO_PI
    )


def recur_step(decay, state, inputs):
    drive_t, valid_t = inputs
    pre = drive_t + decay * state
    state = state + valid_t * (jax.nn.gelu(pre, approximate=False) - state)
    return (state, state)


def back_step(decay, carry, inputs):
    upstream_t, valid_t, pre_t = inputs
    total = upstream_t + carry
    grad_pre = total * valid_t * gelu_slope(pre_t)
    carry = total * (1.0 - valid_t) + grad_pre * decay
    return (carry, grad_pre)


def add_piece(weight, piece):
    return jnp.dot(weight, piece, precision=HIGH, preferred_element_type=jnp.float32)


def weight_columns(grad_pre_norm, piece):
    return jnp.einsum("jf,kf->jk", grad_pre_norm, piece, precision=HIGH)


def split_features(inputs, weights, gains, shifts, decays, biases, lengths, frame_mask, grad_out):
    width, slots = inputs.shape
    clips, frames_len = frame_mask.shape
    frames = jnp.arange(frames_len, dtype=jnp.int32)
    valid_grid = (
        (frames[None, :] < lengths[:, None]) & ((frame_mask == 1) | (frames[None, :] == 0))
    ).astype(jnp.float32)
    valid = valid_grid.reshape(-1)
    valid_row = valid[None, :]
    valid_time = jnp.broadcast_to(valid_grid.T[:, :, None], (frames_len, clips, width)).reshape(
        frames_len, clips * width
    )
    count_local = jnp.sum(valid)

    def to_time(array):
        return jnp.transpose(array.reshape(width, clips, frames_len), (2, 1, 0)).reshape(
            frames_len, clips * width
        )

    def from_time(array):
        return jnp.transpose(array.reshape(frames_len, clips, width), (2, 1, 0)).reshape(
            width, slots
        )

    layer_in = inputs
    saved = []
    for layer_no in range(LAYERS):
        weight = weights[layer_no]
        gathered = lax.all_gather(layer_in, "neuron", axis=0, tiled=True)
        pre_norm = add_piece(weight, gathered)
        first_sum, count = lax.psum((jnp.sum(valid_row * pre_norm, axis=1), count_local), "batch")
        mean = first_sum / count
        centered = pre_norm - mean[:, None]
        var = lax.psum(jnp.sum(valid_row * centered * centered, axis=1), "batch") / count
        inv_std = lax.rsqrt(var + EPS)
        zhat = (pre_norm - mean[:, None]) * inv_std[:, None]
        drive = gains[layer_no][:, None] * zhat + (shifts[layer_no] + biases[layer_no])[:, None]
        drive_time = to_time(drive)
        decay_wide = jnp.tile(decays[layer_no], clips)
        start_state = jnp.zeros((clips * width,), jnp.float32)
        _, states = lax.scan(
            partial(recur_step, decay_wide), start_state, (drive_time, valid_time), unroll=8
        )
        saved.append((gathered, zhat, inv_std, drive_time, states, count))
        layer_in = layer_in + valid_row * from_time(states)
    upstream = grad_out
    grad_parts = [None] * LAYERS
    for layer_no in range(LAYERS - 1, -1, -1):
        gathered, zhat, inv_std, drive_time, states, count = saved[layer_no]
        decay_wide = jnp.tile(decays[layer_no], clips)
        gain = gains[layer_no]
        previous = jnp.concatenate([jnp.zeros_like(states[:1]), states[:-1]], axis=0)
        pre_time = drive_time + decay_wide[None, :] * previous
        grad_state = to_time(valid_row * upstream)
        start_carry = jnp.zeros((clips * width,), jnp.float32)
        _, grad_pre_time = lax.scan(
            partial(back_step, decay_wide),
            start_carry,
            (grad_state, valid_time, pre_time),
            reverse=True,
            unroll=8,
        )
        decay_local = jnp.sum(
            jnp.sum(grad_pre_time * previous, axis=0).reshape(clips, width), axis=0
        )
        grad_pre = from_time(grad_pre_time)
        gain_local = jnp.sum(grad_pre * zhat, axis=1)
        shift_local = jnp.sum(grad_pre, axis=1)
        grad_gain, grad_shift, grad_decay = lax.psum(
            (gain_local, shift_local, decay_local), "batch"
        )
        grad_pre_norm = (gain * inv_std)[:, None] * (
            grad_pre - valid_row * (grad_shift[:, None] + zhat * grad_gain[:, None]) / count
        )
        weight_local = weight_columns(grad_pre_norm, gathered)
        input_terms = jnp.einsum("jk,jf->kf", weights[layer_no], grad_pre_norm, precision=HIGH)
        input_grad = lax.psum_scatter(input_terms, "neuron", scatter_dimension=0, tiled=True)
        grad_weight = lax.psum(weight_local, "batch")
        upstream = upstream + input_grad
        grad_parts[layer_no] = (grad_weight, grad_gain, grad_shift, grad_decay)
    grad_weights = jnp.stack([grad_parts[layer_no][0] for layer_no in range(LAYERS)])
    grad_gains = jnp.stack([grad_parts[layer_no][1] for layer_no in range(LAYERS)])
    grad_shifts = jnp.stack([grad_parts[layer_no][2] for layer_no in range(LAYERS)])
    grad_decays = jnp.stack([grad_parts[layer_no][3] for layer_no in range(LAYERS)])
    return (layer_in, upstream, grad_weights, grad_gains, grad_shifts, grad_decays, grad_shifts)


def solution(mesh):
    if (mesh.shape["batch"], mesh.shape["neuron"]) == (4, 8):
        cut = Mesh(mesh.devices.reshape(2, 2, 2, 2, 2), ("y", "x", "h", "l", "c"))
        batch, neuron, body = ("y", "x"), ("h", "l", "c"), half_features
    else:
        cut, batch, neuron, body = mesh, "batch", "neuron", split_features
    in_specs = (
        P(neuron, batch),
        P(None, neuron, None),
        P(None, neuron),
        P(None, neuron),
        P(None, neuron),
        P(None, neuron),
        P(batch),
        P(batch, None),
        P(neuron, batch),
    )
    out_specs = (
        P(neuron, batch),
        P(neuron, batch),
        P(None, neuron, None),
        P(None, neuron),
        P(None, neuron),
        P(None, neuron),
        P(None, neuron),
    )
    return jax.shard_map(
        body, mesh=cut, in_specs=in_specs, out_specs=out_specs, check_vma=False
    )
```

```python
from functools import partial
import math

import jax
import jax.numpy as jnp
from jax import lax
from jax.experimental import pallas as pl
from jax.experimental.pallas import tpu as pltpu
from jax.sharding import Mesh, PartitionSpec as P

LAYERS = 2
EPS = 1e-05
HIGH = lax.Precision.HIGHEST
ROOT_TWO = math.sqrt(2.0)
ROOT_TWO_PI = math.sqrt(2.0 * math.pi)
F32 = jnp.float32
BF16 = jnp.bfloat16
LANES = 128
VMEM_LIMIT = 24 * 1024 * 1024
SMEM_SPEC = pl.BlockSpec(memory_space=pltpu.SMEM)
VMEM_SPEC = pl.BlockSpec(memory_space=pltpu.VMEM)


FLIP2 = [(0, 1), (1, 0)]
DIAGONAL = [(0, 3), (1, 2), (2, 1), (3, 0)]


def swap_half(array):
    return lax.ppermute(array, "l", FLIP2)


def after(value, *others):
    return lax.optimization_barrier((value, others))[0]


def split(value):
    high = value.astype(BF16)
    return high, (value - high.astype(F32)).astype(BF16)


def dot(a, b, dims):
    return lax.dot_general(a, b, (dims, ((), ())), preferred_element_type=F32)


NT = ((1,), (1,))
NN = ((1,), (0,))


def in_hbm(array):
    return pltpu.with_memory_space_constraint(array, pltpu.HBM)


def call(body, out_shape, hbm_outs=(), **kwargs):
    if hbm_outs:
        out_shape = [
            pltpu.HBM(a.shape, a.dtype) if i in hbm_outs else a for i, a in enumerate(out_shape)
        ]
    return pl.pallas_call(
        body,
        out_shape=out_shape,
        compiler_params=pltpu.CompilerParams(vmem_limit_bytes=VMEM_LIMIT),
        **kwargs,
    )


def cost(flops, byte_count):
    return pl.CostEstimate(flops=int(flops) // 64, bytes_accessed=int(byte_count) // 64, transcendentals=0)


def pack_body(frames, place_ref, in_ref, near_ref, far_ref, turned):
    slots = in_ref.shape[1]
    for start in range(0, slots, LANES):
        turned[start : start + LANES, :] = in_ref[:, start : start + LANES].T
    for rel in range(4):
        first = pl.multiple_of(place_ref[rel] * frames, 8)
        out = (near_ref, far_ref)[rel // 2]
        out[(rel % 2) * frames : (rel % 2 + 1) * frames, :] = turned[pl.ds(first, frames), :]


def pack(place, array, frames, waits=False):
    width, slots = array.shape
    out = jax.ShapeDtypeStruct((2 * frames, width), F32)
    return call(
        partial(pack_body, frames),
        grid=(1,),
        out_shape=[out, out],
        in_specs=[SMEM_SPEC, pl.BlockSpec((width, slots), lambda i: (0, 0))],
        out_specs=[pl.BlockSpec(out.shape, lambda i: (0, 0))] * 2,
        scratch_shapes=[pltpu.VMEM((slots, width), F32)],
        hbm_outs=(0, 1) if waits else (),
        cost_estimate=cost(0, 8 * width * slots),
        name="pack",
    )(place, in_hbm(array))


def part_spec(part, frames):
    array, i = part
    if i is None:
        return pl.BlockSpec(array.shape, lambda *_: (0,) * array.ndim)
    return pl.BlockSpec((frames, array.shape[1]), lambda *_: (i, 0))


def arrays_of(parts):
    return [array for array, _ in parts]


def unpack_body(frames, place_ref, *refs):
    ins, out_ref, turned = refs[:4], refs[4], refs[5]
    slots = out_ref.shape[1]
    for rel in range(4):
        first = pl.multiple_of(place_ref[rel] * frames, 8)
        turned[pl.ds(first, frames), :] = ins[rel][...]
    for start in range(0, slots, LANES):
        out_ref[:, start : start + LANES] = turned[start : start + LANES, :].T


def unpack(place, parts, frames, waited=False):
    width = parts[0][0].shape[1]
    slots = 4 * frames
    return call(
        partial(unpack_body, frames),
        grid=(1,),
        out_shape=jax.ShapeDtypeStruct((width, slots), F32),
        in_specs=[SMEM_SPEC] + [part_spec(part, frames) for part in parts],
        out_specs=pl.BlockSpec((width, slots), lambda i: (0, 0)),
        scratch_shapes=[pltpu.VMEM((slots, width), F32)],
        cost_estimate=cost(0, 8 * width * slots),
        name="unpack",
    )(place, *[in_hbm(a) if waited else a for a in arrays_of(parts)])


def merge_body(kept_ref, come_ref, out_ref):
    frames, columns = kept_ref.shape
    width = columns // 2
    for i in range(2):
        some = slice(i * width, (i + 1) * width)
        out_ref[i * frames : (i + 1) * frames, :] = kept_ref[:, some] + come_ref[:, some]


def merge(kept, half, come):
    frames, columns = come.shape
    return call(
        merge_body,
        grid=(1,),
        out_shape=jax.ShapeDtypeStruct((2 * frames, columns // 2), F32),
        in_specs=[
            pl.BlockSpec((frames, columns), lambda i: (0, half)),
            pl.BlockSpec((frames, columns), lambda i: (0, 0)),
        ],
        out_specs=pl.BlockSpec((2 * frames, columns // 2), lambda i: (0, 0)),
        cost_estimate=cost(0, 12 * frames * columns),
        name="merge",
    )(kept, come)


def project_body(n_parts, n_flat, spots, n_weights, first, with_acc, with_stats, with_params, cols_ref, place_ref, *refs):
    del cols_ref

    def take(n):
        nonlocal refs
        some, refs = refs[:n], refs[n:]
        return some

    parts, flat_parts, weights = take(n_parts), take(n_flat), take(n_weights)
    acc, valid, stats_in, params = take(with_acc), take(with_stats > 0), take(with_stats > 1), take(with_params)
    (out_ref,) = take(1)
    stats, flat = take(with_stats > 0), take(n_flat > 0)
    x_high, x_low, far_ref = refs
    step = pl.program_id(0)
    width = x_high.shape[2]

    @pl.when(step == 0)
    def _():
        for block, part in zip(spots, parts):
            for start in range(0, part.shape[1], width):
                high, low = split(part[:, start : start + width])
                x_high[block + start // width] = high
                x_low[block + start // width] = low
        column = 0
        for part in flat_parts:
            flat[0][:, column : column + part.shape[1]] = part[...]
            column += part.shape[1]
        if with_acc:
            out_ref[...] = acc[0][...]
        else:
            out_ref[...] = jnp.zeros_like(out_ref)

    stacked = jnp.concatenate([x_high[step], x_low[step], x_high[step]], axis=1)
    for block, weight in enumerate(weight_blocks(place_ref, weights, far_ref)):
        w_high, w_low = split(weight)
        columns = slice(block * width, (block + 1) * width)
        out_ref[:, columns] += dot(stacked, jnp.concatenate([w_high, w_high, w_low], axis=1), NT)

    if with_stats:
        (stats_ref,) = stats

        @pl.when(step == pl.num_programs(0) - 1)
        def _():
            if stats_in:
                stats_ref[...] = stats_in[0][...]
            own = jnp.sum(valid[0][...], axis=0, keepdims=True)
            per = width // LANES
            for row in range(out_ref.shape[1] // LANES):
                z = out_ref[:, row * LANES : (row + 1) * LANES]
                total = jnp.sum(valid[0][...] * z, axis=0, keepdims=True)
                centred = valid[0][...] * (z - total / own)
                squares = jnp.sum(centred * centred, axis=0, keepdims=True)
                at = place_ref[first + row // per] * per + row % per
                stats_ref[0, pl.ds(at, 1), :] = total
                stats_ref[1, pl.ds(at, 1), :] = squares
                stats_ref[2, pl.ds(at, 1), :] = own
            if with_params:
                rest = params[0].shape[0] - 8
                stats_ref[3] = params[0][:8, :]
                stats_ref[4] = jnp.zeros_like(stats_ref[4])
                stats_ref[4, :rest, :] = params[0][8:, :]


def weight_specs(weights, layer, pairs=2):
    specs = []
    for weight in weights:
        if weight.ndim == 3:
            shape = (1, weight.shape[1], pairs * weight.shape[1])
            specs.append(pl.BlockSpec(shape, lambda s, cols, *_: (layer, 0, cols[s])))
        else:
            shape = (weight.shape[0], pairs * 4 * weight.shape[0])
            specs.append(pl.BlockSpec(shape, lambda s, cols, *_: (0, cols[s])))
    return specs


def far_scratch(width, pairs=2):
    return pltpu.VMEM((2, width, pairs * width), F32)


def weight_blocks(place_ref, refs, far_ref):
    near = [ref[0] for ref in refs if len(ref.shape) == 3]
    pieces = [ref for ref in refs if len(ref.shape) == 2]
    far = []
    for i in range(len(pieces) // 4):
        for rel, piece in enumerate(pieces[4 * i : 4 * i + 4]):
            rows = piece.shape[0]
            row = 2 * (place_ref[4] ^ (rel // 2)) + (place_ref[5] ^ (rel % 2))
            far_ref[i, pl.ds(pl.multiple_of(row * rows, rows), rows), :] = piece[...]
        far.append(far_ref[i])
    return near + far


def project(
    place, frames, parts, blocks, weights, layer, acc=None, valid=None, stats=None, params=None, flat=()
):
    near = weights[0].ndim == 3
    units = sum(1 if w.ndim == 3 else 0.25 for w in weights)
    width = weights[0].shape[1] if near else 4 * weights[0].shape[0]
    n = blocks.shape[0]
    spots, block = [], 0
    for array, _ in parts:
        spots.append(block)
        block += array.shape[1] // width
    full = pl.BlockSpec(memory_space=pltpu.VMEM)
    in_specs = [part_spec(part, frames) for part in (*parts, *flat)]
    in_specs += weight_specs(weights, layer, 1)
    operands = arrays_of(parts) + arrays_of(flat) + [in_hbm(w) for w in weights]
    array = jax.ShapeDtypeStruct((frames, int(units) * width), F32)
    array_spec = pl.BlockSpec(array.shape, lambda s, cols, place: (0, 0))
    out_shape, out_specs = [array], [array_spec]
    if acc is not None:
        in_specs.append(array_spec)
        operands.append(in_hbm(acc))
    if valid is not None:
        in_specs.append(full)
        operands.append(valid)
        shape = (3 if params is None else 5, 4 * width // LANES, LANES)
        out_shape.append(jax.ShapeDtypeStruct(shape, F32))
        out_specs.append(pl.BlockSpec(shape, lambda s, cols, place: (0, 0, 0)))
    for extra in (stats, params):
        if extra is not None:
            in_specs.append(full)
            operands.append(extra)
    if flat:
        out_shape.append(jax.ShapeDtypeStruct((frames, 4 * width), F32))
        out_specs.append(pl.BlockSpec((frames, 4 * width), lambda s, cols, place: (0, 0)))
    return call(
        partial(
            project_body,
            len(parts),
            len(flat),
            spots,
            len(weights),
            0 if near else 2,
            acc is not None,
            (valid is not None) + (stats is not None),
            params is not None,
        ),
        grid_spec=pltpu.PrefetchScalarGridSpec(
            num_scalar_prefetch=2,
            grid=(n,),
            in_specs=in_specs,
            out_specs=out_specs,
            scratch_shapes=[pltpu.VMEM((n, frames, width), BF16)] * 2 + [far_scratch(width, 1)],
        ),
        out_shape=out_shape,
        hbm_outs=(0, len(out_shape) - 1) if flat else (0,),
        cost_estimate=cost(6 * frames * n * width * units * width, 4 * n * width * units * width),
        name="project",
    )(blocks, place, *operands)


def to_relative(place_ref, spread, rows_ref, value, slot):
    per = value.shape[0] // 4
    spread[...] = value
    for rel in range(4):
        first = place_ref[rel] * per
        for row in range(per):
            rows_ref[slot, rel * per + row : rel * per + row + 1, :] = spread[
                pl.ds(first + row, 1), :
            ]


def tree(values):
    while len(values) > 1:
        values = [a + b for a, b in zip(values[::2], values[1::2])]
    return values[0]


def gathered(ref, slot):
    return [ref[i] for i in range(slot, ref.shape[0], ref.shape[0] // 16)]


def norm_terms(stats_ref):
    each = [gathered(stats_ref, slot) for slot in range(3)]
    totals, squares, owns = each
    count = tree(owns)
    mean = tree(totals) / count
    away = [total / own - mean for total, own in zip(totals, owns)]
    spread = tree([s + n * a * a for s, n, a in zip(squares, owns, away)])
    return count, mean, lax.rsqrt(spread / count + EPS)


CHUNKS = 4


def columns_of(refs, row):
    for ref in refs:
        if row * LANES < ref.shape[1]:
            return ref[:, row * LANES : (row + 1) * LANES]
        row -= ref.shape[1] // LANES


def recur_body(n_z, last, layer, spread_params, place_ref, gate_ref, *refs):
    z_refs, refs = refs[:n_z], refs[n_z:]
    (stats_ref, params_ref, valid_ref, x_ref), refs = refs[:4], refs[4:]
    outs, refs = refs[: 1 + 3 * last], refs[1 + 3 * last :]
    if spread_params:
        state_ref, slope_ref, params_out, rows, spread, held, drive_s, state_s, slope_s = refs
    else:
        state_ref, slope_ref, rows, spread, held, drive_s, state_s, slope_s = refs
    frames, features = x_ref.shape
    blocks = features // LANES
    per = blocks // 4
    chunk = pl.program_id(0)

    @pl.when(chunk == 0)
    def _():
        if spread_params:
            for rel in range(4):
                first = place_ref[rel] * (stats_ref.shape[0] // 16) + 3
                for row in range(LAYERS * 3 * per):
                    at = rel * per + row % per
                    params_out[row // per, at : at + 1, :] = stats_ref[
                        first + row // 8, row % 8 : row % 8 + 1, :
                    ]
            params = [params_out[3 * layer + i] for i in range(3)]
        else:
            params = [params_ref[3 * layer + i] for i in range(3)]
        _, mean, inv_std = norm_terms(stats_ref)
        to_relative(place_ref, spread, rows, mean, 0)
        to_relative(place_ref, spread, rows, inv_std, 1)
        rows[1] = rows[1] * params[0]
        rows[2] = params[1]
        rows[3] = params[2]
        held[...] = jnp.zeros_like(held)

    for row in range(blocks):
        drive_s[row * frames : (row + 1) * frames, :] = (
            columns_of(z_refs, row) - rows[0, row : row + 1, :]
        ) * rows[1, row : row + 1, :] + rows[2, row : row + 1, :]
    decay = rows[3]

    def step(t, state):
        at = pl.ds(t, blocks, stride=frames)
        pre = drive_s[at, :] + decay * state
        half = 0.5 + 0.5 * lax.erf(pre * (1.0 / ROOT_TWO))
        gate = gate_ref[chunk * frames + t] > 0.0
        slope = half + pre * jnp.exp(-0.5 * pre * pre) * (1.0 / ROOT_TWO_PI)
        state = jnp.where(gate, pre * half, state)
        state_s[at, :] = state
        slope_s[at, :] = jnp.where(gate, slope, 0.0)
        return state

    held[...] = lax.fori_loop(0, frames, step, held[...], unroll=8)
    valid = valid_ref[...]
    for row in range(blocks):
        lanes = slice(row * LANES, (row + 1) * LANES)
        state = state_s[row * frames : (row + 1) * frames, :]
        state_ref[:, lanes] = state
        slope_ref[:, lanes] = slope_s[row * frames : (row + 1) * frames, :]
        value = x_ref[:, lanes] + valid * state
        out, at = (outs[row // per], row % per) if last else (outs[0], row)
        out[:, at * LANES : (at + 1) * LANES] = value


def recur(layer, place, gate, z, stats, params, valid, x, last):
    frames, features = x.shape
    blocks = features // LANES
    some = frames // CHUNKS
    whole = lambda array: pl.BlockSpec(array.shape, lambda i: (0,) * array.ndim)
    by_chunk = lambda array: pl.BlockSpec((some, array.shape[1]), lambda i: (i, 0))
    full = jax.ShapeDtypeStruct((frames, features), F32)
    piece = jax.ShapeDtypeStruct((frames, features // 4), F32)
    out_shape = [piece] * 4 if last else [full]
    out_shape += [full, full]
    out_specs = [by_chunk(a) for a in out_shape]
    spread_params = params is None
    if spread_params:
        out_shape.append(jax.ShapeDtypeStruct((3 * LAYERS, blocks, LANES), F32))
        out_specs.append(whole(out_shape[-1]))
        params = valid
    return call(
        partial(recur_body, len(z), last, layer, spread_params),
        grid=(CHUNKS,),
        in_specs=[SMEM_SPEC, SMEM_SPEC]
        + [by_chunk(a) for a in z]
        + [whole(a) for a in (stats, params)]
        + [by_chunk(a) for a in (valid, x)],
        out_specs=out_specs,
        out_shape=out_shape,
        hbm_outs=tuple(range(len(out_shape) - spread_params)) if last else (1, 2),
        scratch_shapes=[
            pltpu.VMEM((4, blocks, LANES), F32),
            pltpu.VMEM((blocks, LANES), F32),
            pltpu.VMEM((blocks, LANES), F32),
        ]
        + [pltpu.VMEM((blocks * some, LANES), F32)] * 3,
        cost_estimate=cost(100 * frames * features, 20 * frames * features),
        name="recur",
    )(place, gate, *[in_hbm(a) for a in z], stats, params, valid, in_hbm(x))


def back_body(n_z, n_ups, spots, layer, place_ref, gate_ref, *refs):
    z_refs, refs = refs[:n_z], refs[n_z:]
    (stats_ref, params_ref), refs = refs[:2], refs[2:]
    ups, (state_ref, slope_ref), refs = refs[:n_ups], refs[n_ups : n_ups + 2], refs[n_ups + 2 :]
    grad_ref, sums_ref, rows, spread, held, up_s, state_s, slope_s = refs
    frames, features = state_ref.shape
    blocks = features // LANES
    per = blocks // 4
    tall = frames + 8
    step_no = pl.program_id(0)
    chunk = pl.num_programs(0) - 1 - step_no

    @pl.when(step_no == 0)
    def _():
        _, mean, inv_std = norm_terms(stats_ref)
        to_relative(place_ref, spread, rows, mean, 0)
        to_relative(place_ref, spread, rows, inv_std, 1)
        held[...] = jnp.zeros_like(held)

    for row in range(blocks):
        lanes = slice(row * LANES, (row + 1) * LANES)
        base = row * frames
        up = None
        for (_, column), part in zip(spots, ups):
            if column <= row * LANES < column + part.shape[1]:
                value = part[:, row * LANES - column : (row + 1) * LANES - column]
                up = value if up is None else up + value
        up_s[base : base + frames, :] = up
        state_s[row * tall : row * tall + 8, :] = jnp.zeros((8, LANES), F32)
        state_s[row * tall + 8 : (row + 1) * tall, :] = state_ref[:, lanes]
        slope_s[base : base + frames, :] = slope_ref[:, lanes]
    decay = params_ref[3 * layer + 2]

    def step(i, carry):
        t = frames - 1 - i
        at = pl.ds(t, blocks, stride=frames)
        slope = slope_s[at, :]
        gate = gate_ref[chunk * frames + t]
        total = gate * up_s[at, :] + carry
        up_s[at, :] = total * slope
        return total * (slope * decay + (1.0 - gate))

    held[0] = lax.fori_loop(0, frames, step, held[0], unroll=8)
    held[4] += held[1] * state_s[pl.ds(tall - 1, blocks, stride=tall), :]
    held[1] = up_s[pl.ds(0, blocks, stride=frames), :]
    for row in range(blocks):
        lanes = slice(row * LANES, (row + 1) * LANES)
        grad = up_s[row * frames : (row + 1) * frames, :]
        grad_ref[:, lanes] = grad
        zhat = (columns_of(z_refs, row) - rows[0, row : row + 1, :]) * rows[1, row : row + 1, :]
        before = state_s[row * tall + 7 : row * tall + 7 + frames, :]
        for slot, value in enumerate((grad * zhat, grad, grad * before)):
            held[2 + slot, row : row + 1, :] += jnp.sum(value, axis=0, keepdims=True)

    @pl.when(chunk == 0)
    def _():
        for row in range(blocks):
            at = place_ref[row // per] * per + row % per
            for slot in range(3):
                sums_ref[slot, pl.ds(at, 1), :] = held[2 + slot, row : row + 1, :]


def spots_of_sum(parts, width):
    spots, column = [], 0
    for array, _ in parts:
        spots.append((0, column % (4 * width)))
        column += array.shape[1]
    return spots


def back(layer, place, gate, z, stats, params, ups, states, slopes):
    frames, features = states.shape
    width = features // 4
    blocks = features // LANES
    some = frames // CHUNKS
    whole = lambda array: pl.BlockSpec(array.shape, lambda i: (0,) * array.ndim)

    def by_chunk(array, first=0):
        return pl.BlockSpec(
            (some, array.shape[1]), lambda i: ((first or 0) * CHUNKS + CHUNKS - 1 - i, 0)
        )

    out_shape = [
        jax.ShapeDtypeStruct((frames, features), F32),
        jax.ShapeDtypeStruct((3, blocks, LANES), F32),
    ]
    return call(
        partial(back_body, len(z), len(ups), spots_of_sum(ups, width), layer),
        grid=(CHUNKS,),
        in_specs=[SMEM_SPEC] * 2
        + [by_chunk(a) for a in z]
        + [whole(a) for a in (stats, params)]
        + [by_chunk(*up) for up in ups]
        + [by_chunk(a) for a in (states, slopes)],
        out_specs=[by_chunk(out_shape[0]), whole(out_shape[1])],
        out_shape=out_shape,
        scratch_shapes=[
            pltpu.VMEM((2, blocks, LANES), F32),
            pltpu.VMEM((blocks, LANES), F32),
            pltpu.VMEM((5, blocks, LANES), F32),
            pltpu.VMEM((blocks * some, LANES), F32),
            pltpu.VMEM((blocks * (some + 8), LANES), F32),
            pltpu.VMEM((blocks * some, LANES), F32),
        ],
        cost_estimate=cost(30 * frames * features, 20 * frames * features),
        name="back",
    )(
        place,
        gate,
        *[in_hbm(a) for a in z],
        stats,
        params,
        *arrays_of(ups),
        in_hbm(states),
        in_hbm(slopes),
    )


def input_terms(high_s, low_s, weights):
    left, right = [], []
    for block, weight in enumerate(weights):
        w_high, w_low = split(weight)
        left += [high_s[block], low_s[block], high_s[block]]
        right += [w_high, w_high, w_low]
    return dot(jnp.concatenate(left, axis=1), jnp.concatenate(right, axis=0), NN)


def norm_back_body(n_z, split_terms, layer, cols_ref, place_ref, grad_ref, *refs):
    del cols_ref
    z_refs, refs = refs[:n_z], refs[n_z:]
    params_ref, valid_ref, stats_ref, sums_ref, *refs = refs
    weights, refs = refs[:10], refs[10:]
    if split_terms:
        out_ref, leave_ref, near_term_ref, far_term_ref, sums_out_ref, *refs = refs
        term_refs, starts = (far_term_ref, near_term_ref), (0, 0)
    else:
        out_ref, leave_ref, term_ref, sums_out_ref, *refs = refs
        term_refs, starts = (term_ref, term_ref), (2 * grad_ref.shape[1] // 4, 0)
    rows, spread, high_s, low_s, far_ref = refs
    blocks = grad_ref.shape[1] // LANES
    width = high_s.shape[2]
    per = width // LANES

    @pl.when(pl.program_id(0) == 0)
    def _():
        count, mean, inv_std = norm_terms(stats_ref)
        to_relative(place_ref, spread, rows, mean, 0)
        to_relative(place_ref, spread, rows, inv_std, 1)
        rows[2] = rows[1] * params_ref[3 * layer]
        sums = [tree(gathered(sums_ref, slot)) for slot in range(3)]
        for slot in range(3):
            sums_out_ref[slot] = sums[slot]
        to_relative(place_ref, spread, rows, sums[0] / count, 3)
        to_relative(place_ref, spread, rows, sums[1] / count, 4)
        valid = valid_ref[...]
        for row in range(blocks):
            lanes = slice(row * LANES, (row + 1) * LANES)
            one = lambda slot: rows[slot, row : row + 1, :]
            zhat = (columns_of(z_refs, row) - one(0)) * one(1)
            value = one(2) * (grad_ref[:, lanes] - valid * (one(4) + zhat * one(3)))
            out_ref[:, lanes] = value
            if (row // per) % 2:
                at = (row // per // 2) * width + (row % per) * LANES
                leave_ref[:, at : at + LANES] = value
            high, low = split(value)
            inner = slice((row % per) * LANES, (row % per + 1) * LANES)
            high_s[row // per, :, inner] = high
            low_s[row // per, :, inner] = low

    value = input_terms(high_s, low_s, weight_blocks(place_ref, weights, far_ref))
    for step, (term_ref, first) in enumerate(zip(term_refs, starts)):

        @pl.when(pl.program_id(0) == step)
        def _():
            for pair in range(2):
                at = pl.multiple_of(((place_ref[0] & 1) ^ pair) * width, width)
                term_ref[:, pl.ds(first + at, width)] = value[
                    :, pair * width : (pair + 1) * width
                ]


def norm_back(columns, place, grad, z, params, valid, stats, sums, weights, layer, split_terms):
    frames, features = grad.shape
    width = features // 4
    blocks = features // LANES
    whole = lambda array: pl.BlockSpec(array.shape, lambda s, cols, place: (0,) * array.ndim)
    operands = [grad, *[in_hbm(a) for a in z], params, valid, stats, sums]
    full = jax.ShapeDtypeStruct((frames, features), F32)
    half = jax.ShapeDtypeStruct((frames, 2 * width), F32)
    terms = [half, half] if split_terms else [full]
    out_shape = [full, half, *terms, jax.ShapeDtypeStruct((3, blocks, LANES), F32)]
    return call(
        partial(norm_back_body, len(z), split_terms, layer),
        grid_spec=pltpu.PrefetchScalarGridSpec(
            num_scalar_prefetch=2,
            grid=(2,),
            in_specs=[whole(a) for a in operands] + weight_specs(weights, layer),
            out_specs=[whole(a) for a in out_shape],
            scratch_shapes=[
                pltpu.VMEM((5, blocks, LANES), F32),
                pltpu.VMEM((blocks, LANES), F32),
                pltpu.VMEM((4, frames, width), BF16),
                pltpu.VMEM((4, frames, width), BF16),
                far_scratch(width),
            ],
        ),
        out_shape=out_shape,
        hbm_outs=(0,),
        cost_estimate=cost(6 * frames * features * features, 4 * features * features),
        name="norm_back",
    )(columns, place, *operands, *[in_hbm(w) for w in weights])


def own_terms_body(n_ups, spots, cols_ref, place_ref, grad_ref, *refs):
    del cols_ref
    ups, refs = refs[:n_ups], refs[n_ups:]
    weights, refs = refs[:10], refs[10:]
    out_ref, high_s, low_s, far_ref = refs
    width = high_s.shape[2]
    step = pl.program_id(0)

    @pl.when(step == 0)
    def _():
        for block in range(4):
            high, low = split(grad_ref[:, block * width : (block + 1) * width])
            high_s[block] = high
            low_s[block] = low

    value = input_terms(high_s, low_s, weight_blocks(place_ref, weights, far_ref))
    for pair in range(2):
        at = pl.multiple_of(((place_ref[0] & 1) ^ pair) * width, width)
        out_ref[:, pl.ds(at, width)] = value[:, pair * width : (pair + 1) * width]
    for half in range(2):

        @pl.when(step == half)
        def _():
            first = 2 * half * width
            for (_, column), up in zip(spots, ups):
                low = max(column, first)
                high = min(column + up.shape[1], first + 2 * width)
                if low < high:
                    out_ref[:, low - first : high - first] += up[:, low - column : high - column]


def own_terms(columns, place, grad, ups, weights, layer):
    frames, features = grad.shape
    width = features // 4
    whole = lambda array: pl.BlockSpec(array.shape, lambda s, cols, place: (0,) * array.ndim)
    step_block = pl.BlockSpec((frames, 2 * width), lambda s, cols, place: (0, s))
    return call(
        partial(own_terms_body, len(ups), spots_of_sum(ups, width)),
        grid_spec=pltpu.PrefetchScalarGridSpec(
            num_scalar_prefetch=2,
            grid=(2,),
            in_specs=[whole(grad)]
            + [part_spec(up, frames) for up in ups]
            + weight_specs(weights, layer),
            out_specs=step_block,
            scratch_shapes=[pltpu.VMEM((4, frames, width), BF16)] * 2 + [far_scratch(width)],
        ),
        out_shape=jax.ShapeDtypeStruct((frames, features), F32),
        cost_estimate=cost(6 * frames * features * features, 4 * features * features),
        name="own_terms",
    )(columns, place, in_hbm(grad), *arrays_of(ups), *[in_hbm(w) for w in weights])


def prepare_body(lists_ref, place_ref, own_ref, near_ref, high_ref, low_ref):
    del lists_ref
    padded = high_ref.shape[0] // 2
    width = high_ref.shape[1] // 2
    for clip, part in enumerate((own_ref, near_ref)):
        rows = part.shape[0]
        for dc in range(2):
            at = pl.multiple_of((place_ref[6] ^ clip ^ dc) * width, width)
            high, low = split(part[:, dc * width : (dc + 1) * width])
            high_ref[clip * padded : clip * padded + rows, pl.ds(at, width)] = high
            low_ref[clip * padded : clip * padded + rows, pl.ds(at, width)] = low
        zeros = jnp.zeros((padded - rows, 2 * width), BF16)
        high_ref[clip * padded + rows : (clip + 1) * padded, :] = zeros
        low_ref[clip * padded + rows : (clip + 1) * padded, :] = zeros


def prepare(place, own, near):
    frames, features = own.shape
    width = features // 4
    padded = -(-frames // LANES) * LANES
    in_spec = pl.BlockSpec((frames, 2 * width), lambda s, *_: (0, s))
    out = jax.ShapeDtypeStruct((2 * padded, features), BF16)
    out_spec = pl.BlockSpec((2 * padded, 2 * width), lambda s, order, place: (0, order[s]))
    order = jnp.stack([place[0] >> 1, 1 - (place[0] >> 1)])
    return call(
        prepare_body,
        grid_spec=pltpu.PrefetchScalarGridSpec(
            num_scalar_prefetch=2,
            grid=(2,),
            in_specs=[in_spec, in_spec],
            out_specs=[out_spec, out_spec],
        ),
        out_shape=[out, out],
        hbm_outs=(0, 1),
        cost_estimate=cost(0, 16 * frames * features),
        name="prepare",
    )(order, place, in_hbm(own), in_hbm(near))


def product(g_high, g_low, x_high, x_low):
    return dot(g_high, x_high, NN) + (dot(g_high, x_low, NN) + dot(g_low, x_high, NN))


def weight_body(turn, place_ref, *refs):
    if turn:
        grad_ref, near_ref, x_high, x_low, kept, sent, g_high, g_low, t_high, t_low = refs

        @pl.when(pl.program_id(0) == 0)
        def _():
            frames, features = grad_ref.shape
            width = features // 4
            rows = width // 4
            padded = t_high.shape[1] // 2
            t_high[...] = jnp.zeros_like(t_high)
            t_low[...] = jnp.zeros_like(t_low)
            for clip in range(2):
                for dh in range(2):
                    if clip == 0:
                        part = grad_ref[:, 2 * dh * width : (2 * dh + 1) * width]
                    else:
                        part = near_ref[:, dh * width : (dh + 1) * width]
                    high, low = split(part.T)
                    at = (
                        slice(dh * width, (dh + 1) * width),
                        slice(clip * padded, clip * padded + frames),
                    )
                    t_high[at] = high
                    t_low[at] = low
            for group in range(8):
                first, second, dh = group // 4, group // 2 % 2, group % 2
                core = place_ref[6]
                y = place_ref[4] ^ (first * core + second * (1 - core))
                x = place_ref[5] ^ (first * (1 - core) + second * core)
                at = pl.multiple_of(dh * width + (2 * y + x) * rows, rows)
                g_high[group * rows : (group + 1) * rows, :] = t_high[pl.ds(at, rows), :]
                g_low[group * rows : (group + 1) * rows, :] = t_low[pl.ds(at, rows), :]

    else:
        g_high, g_low, x_high, x_low, kept, sent = refs
    half = g_high.shape[0] // 2
    value = product(g_high[...], g_low[...], x_high[...], x_low[...])
    kept[...] = value[:half].reshape(kept.shape)
    sent[...] = value[half:].reshape(sent.shape)


def weight_rows(side, place, grads, x_split, width):
    turn = side == 0
    whole = lambda array: pl.BlockSpec(array.shape, lambda s, place: (0,) * array.ndim)
    x_spec = pl.BlockSpec((x_split[0].shape[0], width), lambda s, place: (0, s))
    shape = (2, 2, width // 4, 4 * width)
    out_shape = [jax.ShapeDtypeStruct(shape, F32)] * 2
    out_specs = [pl.BlockSpec(shape[:3] + (width,), lambda s, place: (0, 0, 0, s))] * 2
    scratch = []
    if turn:
        turned = (2 * width, x_split[0].shape[0])
        out_shape += [jax.ShapeDtypeStruct(turned, BF16)] * 2
        out_specs += [whole(out_shape[-1])] * 2
        scratch = [pltpu.VMEM(turned, BF16)] * 2
    return call(
        partial(weight_body, turn),
        grid_spec=pltpu.PrefetchScalarGridSpec(
            num_scalar_prefetch=1,
            grid=(4,),
            in_specs=[whole(a) for a in grads] + [x_spec] * 2,
            out_specs=out_specs,
            scratch_shapes=scratch,
        ),
        out_shape=out_shape,
        hbm_outs=(0,),
        cost_estimate=cost(12 * x_split[0].shape[0] * width * 4 * width, 4 * 8 * width * width),
        name="weight_rows",
    )(place, *([in_hbm(grads[0]), grads[1]] if turn else grads), *[in_hbm(x) for x in x_split])


def step_body(n, widths, cut, *refs):
    ins, outs = refs[: 2 * n], refs[2 * n :]
    starts = [sum(widths[:i]) for i in range(len(widths))]
    column = 0
    for i in range(n):
        total = ins[2 * i][...] + ins[2 * i + 1][...]
        end = column + total.shape[-1]
        for j, (start, columns) in enumerate(zip(starts, widths)):
            low, high = max(start, column), min(start + columns, end)
            if low < high:
                to = (Ellipsis, slice(low - start, high - start))
                piece = total[..., low - column : high - column]
                if cut:
                    outs[2 * j][to] = piece[0]
                    outs[2 * j + 1][to] = piece[1]
                else:
                    outs[j][to] = piece
        column = end


def step_of(*pairs, cut=True, widths=None):
    shape = list(pairs[0][0].shape)
    widths = widths or [sum(pair[0].shape[-1] for pair in pairs)]
    outs = []
    for columns in widths:
        shape[-1] = columns
        out = jax.ShapeDtypeStruct(tuple(shape[1:] if cut else shape), F32)
        outs += [out] * (1 + cut)
    whole = lambda array: pl.BlockSpec(array.shape, lambda i: (0,) * array.ndim)
    operands = [array for pair in pairs for array in pair]
    return call(
        partial(step_body, len(pairs), widths, cut),
        grid=(1,),
        in_specs=[whole(a) for a in operands],
        out_specs=[whole(a) for a in outs],
        out_shape=outs,
        cost_estimate=cost(0, 4 * sum(a.size for a in operands)),
        name="reduction_step",
    )(*operands)


def plane_swap(array, step):
    pairs = []
    for i in range(8):
        over_x = (i % 2 == 0) == (step == 0)
        pairs.append((i, i ^ 2 if over_x else i ^ 4))
    return lax.ppermute(array, ("y", "x", "c"), pairs)


def plane_gather(share, *before):
    first = plane_swap(share, 0)
    second = plane_swap(share, 1)
    return [share, second, first, plane_swap(after(first, *before), 1)]


def assemble_body(by_core, place_ref, *refs):
    out_ref = refs[-1]
    core = place_ref[6] if by_core else 1
    rows, columns = refs[0].shape
    quarter = columns // 4
    for i in range(4):
        first, second = i // 2, i % 2
        y = place_ref[4] ^ (first * core + second * (1 - core))
        x = place_ref[5] ^ (first * (1 - core) + second * core)
        at = pl.multiple_of((2 * y + x) * rows, rows)
        for side in range(2):
            for h in range(2):
                to = pl.multiple_of((2 * h + (place_ref[7] ^ side)) * quarter, quarter)
                some = slice((2 * side + h) * quarter, (2 * side + h + 1) * quarter)
                out_ref[0, pl.ds(at, rows), pl.ds(to, quarter)] = refs[i][:, some]


def assemble(place, pieces, layer, onto=None, by_core=True):
    rows, columns = 4 * pieces[0].shape[0], pieces[0].shape[1]
    aliases, extra, extra_specs = {}, [], []
    if onto is not None:
        aliases, extra = {1 + len(pieces): 0}, [onto]
        extra_specs = [pl.BlockSpec(memory_space=pl.ANY)]
    (out,) = call(
        partial(assemble_body, by_core),
        grid=(1,),
        out_shape=[jax.ShapeDtypeStruct((LAYERS, rows, columns), F32)],
        hbm_outs=(0,),
        in_specs=[SMEM_SPEC]
        + [pl.BlockSpec(p.shape, lambda i: (0, 0)) for p in pieces]
        + extra_specs,
        out_specs=[pl.BlockSpec((1, rows, columns), lambda i: (layer, 0, 0))],
        input_output_aliases=aliases,
        cost_estimate=cost(0, 8 * rows * columns),
        name="assemble",
    )(place, *[p if extra else in_hbm(p) for p in pieces], *extra)
    return out


def half_features(inputs, weights, gains, shifts, decays, biases, lengths, frame_mask, grad_out):
    width, slots = inputs.shape
    clips, frames = frame_mask.shape
    depth = weights.shape[2]
    blocks = 4 * width // LANES
    y, x, h, l, c = (lax.axis_index(name) for name in ("y", "x", "h", "l", "c"))
    b = 2 * y + x
    numbers = [2 * (h ^ (rel // 2)) + (c ^ (rel % 2)) for rel in range(4)] + [y, x, c, l]
    place = jnp.stack(numbers).astype(jnp.int32)
    own_blocks, other_blocks = (
        jnp.stack(
            [2 * (2 * (h ^ (rel // 2)) + half) + (c ^ (rel % 2)) for rel in range(4)]
        ).astype(jnp.int32)
        for half in (l, 1 - l)
    )
    own_columns = jnp.stack([2 * h + l, 2 * (1 - h) + l]).astype(jnp.int32)
    other_columns = jnp.stack([2 * (1 - h) + 1 - l, 2 * h + 1 - l]).astype(jnp.int32)
    rows = width // 4

    clip = 2 * h + c
    seen = lax.dynamic_index_in_dim(frame_mask, clip, 0, keepdims=False)
    length = lax.dynamic_index_in_dim(lengths, clip, 0, keepdims=False)
    moments = jnp.arange(frames, dtype=jnp.int32)
    gate = ((moments < length) & ((seen == 1) | (moments == 0))).astype(F32)
    valid = jnp.broadcast_to(gate[:, None], (frames, LANES))

    def far_share(layer):
        return lax.dynamic_slice(weights, (layer, b * rows, 0), (1, rows, depth))[0]

    def over_h(array):
        return lax.ppermute(array, "h", FLIP2)

    def over_c(array):
        return lax.ppermute(array, "c", FLIP2)

    def over_second(array):
        return plane_swap(array, 1)

    def four_of(near_rows, far_rows):
        return [
            (near_rows, 0),
            (over_c(near_rows), 1),
            (far_rows, 0),
            (over_c(far_rows), 1),
        ]

    def four_of_plane(share):
        both = lax.ppermute(share, ("y", "x"), DIAGONAL)
        return [share, lax.ppermute(share, "x", FLIP2), lax.ppermute(share, "y", FLIP2), both]

    near = over_c(weights)
    share = far_share(0)
    close, away = pack(place, after(inputs, share), frames)
    share = over_h(share)
    away = over_h(away)
    other_close = swap_half(close)
    up_close, up_away = pack(place, after(grad_out, close), frames, waits=True)
    share = after(share, up_close, valid, near, other_close)
    pieces = four_of_plane(share)
    away = after(away, pieces[1:])
    half_weights = [[weights, near, *pieces, *map(over_c, after(pieces, away))]]
    own = four_of(after(close, away), away)
    other_away = swap_half(away)
    others = [(other_close, 0), (over_c(other_close), 1)]
    params = jnp.stack([gains, shifts + biases, decays], axis=1)
    own_params = params.reshape(LAYERS * 3 * width // LANES, LANES)
    params = None

    def gather(array, axes):
        return lax.all_gather(array, axes, tiled=True)

    weight = half_weights[0]
    early = jnp.concatenate([own_blocks, other_blocks[:2]])
    z, own_flat = project(place, frames, own + others, early, weight, 0, flat=own)
    others += [(other_away, 0), (over_c(after(other_away, z)), 1)]
    z, stats, other_flat = project(
        place,
        frames,
        others[2:],
        other_blocks[2:],
        weight,
        0,
        z,
        valid,
        params=own_params,
        flat=others,
    )
    z = [z]
    stats = gather(stats, ("h", "c"))
    share = over_c(lax.ppermute(after(far_share(1), stats), ("h", "c"), DIAGONAL))
    stats = gather(stats, ("y", "x"))
    x, states, slopes, params = recur(0, place, gate, z, stats, None, valid, own_flat, False)
    own_near, other_near = over_c(after(own_flat, z[0])), over_c(after(other_flat, z[0]))
    x_near = over_c(x)
    own_split = prepare(place, after(own_flat, x_near), own_near)
    other_split = prepare(place, after(other_flat, x_near), other_near)
    saved = [(own_split, other_split, z, stats, states, slopes)]

    pieces = four_of_plane(after(share, slopes, own_near, other_near))
    near = [weights, near]
    other = swap_half(x)
    x_own = after(x, own_split[0], other_split[0])
    z, *_ = project(place, frames, [(x_own, None)], own_blocks, near, 1)
    own_split = prepare(place, after(x, z), x_near)
    far = [*pieces, *map(over_c, after(pieces, own_split[0]))]
    up_away = over_h(after(up_away, other, own_split[0]))
    half_weights.append(near + far)
    z, stats = project(place, frames, [(other, None)], other_blocks, near, 1, z, valid)
    both = jnp.concatenate([own_blocks, other_blocks])
    z_far, stats = project(
        place,
        frames,
        [(x, None), (other, None)],
        both,
        far,
        1,
        None,
        valid,
        stats,
    )
    z = [z, z_far]
    stats = gather(gather(stats, ("y", "x")), ("h", "c"))
    upstream = four_of(up_close, after(up_away, stats))
    *output, states, slopes = recur(1, place, gate, z, stats, params, valid, x, True)
    other_near = over_c(after(other, slopes))
    saved.append((own_split, (other, other_near), z, stats, states, slopes))
    diagonal = over_c(over_h(output[3]))

    ups = upstream
    results = [None] * LAYERS
    for layer in range(LAYERS - 1, -1, -1):
        own_split, other_split, z, stats, states, slopes = saved[layer]
        weight = half_weights[layer]
        grad_pre, sums = back(layer, place, gate, z, stats, params, ups, states, slopes)
        sums = gather(sums, ("y", "x"))
        if layer == 0:
            come[0] = after(come[0], sums)
            later, go = step_of((in_hbm(stay[0]), come[0]), (in_hbm(stay[1]), come[1]))
            sums = after(sums, later)
            go = over_second(go)
        sums = gather(sums, ("h", "c"))
        if layer > 0:
            away = over_c(lax.ppermute(after(output[2], sums), ("h", "c"), DIAGONAL))
        grad_z, leaving, *terms, sums = norm_back(
            other_columns, place, grad_pre, z, params, valid, stats, sums, weight, layer,
            layer == 0,
        )
        leaving = over_c(leaving)
        if layer > 0:
            received = [swap_half(terms[0])]
            other_split = prepare(place, *after(other_split, grad_z))
            leaving = after(leaving, diagonal, away, other_split[0])
        else:
            received = [None, swap_half(terms[1])]
            later, go = step_of((later, after(go, grad_z)))
            leaving = after(leaving, later)
            go = lax.ppermute(go, ("h", "c"), DIAGONAL)
            later = (later, go)
        *first, g_high, g_low = weight_rows(0, place, (grad_z, leaving), own_split, width)
        turned = (g_high, g_low)
        come = [plane_swap(first[1], 0)]
        if layer > 0:
            output = [(a, 0) for a in (output[0], over_c(output[1]), away, diagonal)]
        else:
            received[0] = swap_half(after(terms[0], received[1]))
        second = weight_rows(1, place, turned, other_split, width)
        come.append(plane_swap(second[1], 0))
        stay = (first[0], second[0])
        kept = own_terms(own_columns, place, after(grad_z, second[0]), ups, weight, layer)
        ups = [(kept, None)] + [(r, None) for r in received]
        results[layer] = lax.dynamic_index_in_dim(
            sums.reshape(3, 4, width), clip, axis=1, keepdims=False
        )

    sums = jnp.stack(results)
    sums = [sums[:, 0], sums[:, 1], sums[:, 2]]
    away = merge(kept, 1, received[1])
    later = (later[0], over_c(after(later[1], away)))
    come[0] = after(come[0], sums, later[1])
    away = over_h(away)
    far = over_c(after(away, received[0]))
    total, go = step_of((in_hbm(stay[0]), come[0]), (in_hbm(stay[1]), come[1]))
    go = over_second(go)
    (later,) = step_of(later, cut=False)
    later = four_of_plane(later)
    total, go = step_of((total, after(go, far)))
    go = over_h(go)
    output = unpack(place, [(after(array, total), i) for array, i in output], frames, waited=True)
    close = merge(kept, 0, after(received[0], output))
    grad_in = [(close, 0), (over_c(close[frames:]), 0), (away, 0), (far, 1)]
    grad_in = unpack(place, grad_in, frames)
    grad_weights = assemble(place, after(later, grad_in), 1, by_core=False)
    (share,) = step_of((total, after(go, grad_weights)), cut=False)
    gathered = plane_gather(share)
    grad_weights = assemble(place, gathered, 0, grad_weights)
    return (output, grad_in, grad_weights, *sums, sums[1])


def gelu_slope(value):
    return (
        0.5 * (1.0 + jax.scipy.special.erf(value / ROOT_TWO))
        + value * jnp.exp(-0.5 * value * value) / ROOT_TWO_PI
    )


def recur_step(decay, state, inputs):
    drive_t, valid_t = inputs
    pre = drive_t + decay * state
    state = state + valid_t * (jax.nn.gelu(pre, approximate=False) - state)
    return (state, state)


def back_step(decay, carry, inputs):
    upstream_t, valid_t, pre_t = inputs
    total = upstream_t + carry
    grad_pre = total * valid_t * gelu_slope(pre_t)
    carry = total * (1.0 - valid_t) + grad_pre * decay
    return (carry, grad_pre)


def add_piece(weight, piece):
    return jnp.dot(weight, piece, precision=HIGH, preferred_element_type=jnp.float32)


def weight_columns(grad_pre_norm, piece):
    return jnp.einsum("jf,kf->jk", grad_pre_norm, piece, precision=HIGH)


def split_features(inputs, weights, gains, shifts, decays, biases, lengths, frame_mask, grad_out):
    width, slots = inputs.shape
    clips, frames_len = frame_mask.shape
    frames = jnp.arange(frames_len, dtype=jnp.int32)
    valid_grid = (
        (frames[None, :] < lengths[:, None]) & ((frame_mask == 1) | (frames[None, :] == 0))
    ).astype(jnp.float32)
    valid = valid_grid.reshape(-1)
    valid_row = valid[None, :]
    valid_time = jnp.broadcast_to(valid_grid.T[:, :, None], (frames_len, clips, width)).reshape(
        frames_len, clips * width
    )
    count_local = jnp.sum(valid)

    def to_time(array):
        return jnp.transpose(array.reshape(width, clips, frames_len), (2, 1, 0)).reshape(
            frames_len, clips * width
        )

    def from_time(array):
        return jnp.transpose(array.reshape(frames_len, clips, width), (2, 1, 0)).reshape(
            width, slots
        )

    layer_in = inputs
    saved = []
    for layer_no in range(LAYERS):
        weight = weights[layer_no]
        gathered = lax.all_gather(layer_in, "neuron", axis=0, tiled=True)
        pre_norm = add_piece(weight, gathered)
        first_sum, count = lax.psum((jnp.sum(valid_row * pre_norm, axis=1), count_local), "batch")
        mean = first_sum / count
        centered = pre_norm - mean[:, None]
        var = lax.psum(jnp.sum(valid_row * centered * centered, axis=1), "batch") / count
        inv_std = lax.rsqrt(var + EPS)
        zhat = (pre_norm - mean[:, None]) * inv_std[:, None]
        drive = gains[layer_no][:, None] * zhat + (shifts[layer_no] + biases[layer_no])[:, None]
        drive_time = to_time(drive)
        decay_wide = jnp.tile(decays[layer_no], clips)
        start_state = jnp.zeros((clips * width,), jnp.float32)
        _, states = lax.scan(
            partial(recur_step, decay_wide), start_state, (drive_time, valid_time), unroll=8
        )
        saved.append((gathered, zhat, inv_std, drive_time, states, count))
        layer_in = layer_in + valid_row * from_time(states)
    upstream = grad_out
    grad_parts = [None] * LAYERS
    for layer_no in range(LAYERS - 1, -1, -1):
        gathered, zhat, inv_std, drive_time, states, count = saved[layer_no]
        decay_wide = jnp.tile(decays[layer_no], clips)
        gain = gains[layer_no]
        previous = jnp.concatenate([jnp.zeros_like(states[:1]), states[:-1]], axis=0)
        pre_time = drive_time + decay_wide[None, :] * previous
        grad_state = to_time(valid_row * upstream)
        start_carry = jnp.zeros((clips * width,), jnp.float32)
        _, grad_pre_time = lax.scan(
            partial(back_step, decay_wide),
            start_carry,
            (grad_state, valid_time, pre_time),
            reverse=True,
            unroll=8,
        )
        decay_local = jnp.sum(
            jnp.sum(grad_pre_time * previous, axis=0).reshape(clips, width), axis=0
        )
        grad_pre = from_time(grad_pre_time)
        gain_local = jnp.sum(grad_pre * zhat, axis=1)
        shift_local = jnp.sum(grad_pre, axis=1)
        grad_gain, grad_shift, grad_decay = lax.psum(
            (gain_local, shift_local, decay_local), "batch"
        )
        grad_pre_norm = (gain * inv_std)[:, None] * (
            grad_pre - valid_row * (grad_shift[:, None] + zhat * grad_gain[:, None]) / count
        )
        weight_local = weight_columns(grad_pre_norm, gathered)
        input_terms = jnp.einsum("jk,jf->kf", weights[layer_no], grad_pre_norm, precision=HIGH)
        input_grad = lax.psum_scatter(input_terms, "neuron", scatter_dimension=0, tiled=True)
        grad_weight = lax.psum(weight_local, "batch")
        upstream = upstream + input_grad
        grad_parts[layer_no] = (grad_weight, grad_gain, grad_shift, grad_decay)
    grad_weights = jnp.stack([grad_parts[layer_no][0] for layer_no in range(LAYERS)])
    grad_gains = jnp.stack([grad_parts[layer_no][1] for layer_no in range(LAYERS)])
    grad_shifts = jnp.stack([grad_parts[layer_no][2] for layer_no in range(LAYERS)])
    grad_decays = jnp.stack([grad_parts[layer_no][3] for layer_no in range(LAYERS)])
    return (layer_in, upstream, grad_weights, grad_gains, grad_shifts, grad_decays, grad_shifts)


def solution(mesh):
    if (mesh.shape["batch"], mesh.shape["neuron"]) == (4, 8):
        cut = Mesh(mesh.devices.reshape(2, 2, 2, 2, 2), ("y", "x", "h", "l", "c"))
        batch, neuron, body = ("y", "x"), ("h", "l", "c"), half_features
    else:
        cut, batch, neuron, body = mesh, "batch", "neuron", split_features
    in_specs = (
        P(neuron, batch),
        P(None, neuron, None),
        P(None, neuron),
        P(None, neuron),
        P(None, neuron),
        P(None, neuron),
        P(batch),
        P(batch, None),
        P(neuron, batch),
    )
    out_specs = (
        P(neuron, batch),
        P(neuron, batch),
        P(None, neuron, None),
        P(None, neuron),
        P(None, neuron),
        P(None, neuron),
        P(None, neuron),
    )
    return jax.shard_map(
        body, mesh=cut, in_specs=in_specs, out_specs=out_specs, check_vma=False
    )
```

```python
from functools import partial
import math

import jax
import jax.numpy as jnp
from jax import lax
from jax.experimental import pallas as pl
from jax.experimental.pallas import tpu as pltpu
from jax.sharding import Mesh, PartitionSpec as P

LAYERS = 2
EPS = 1e-05
HIGH = lax.Precision.HIGHEST
ROOT_TWO = math.sqrt(2.0)
ROOT_TWO_PI = math.sqrt(2.0 * math.pi)
F32 = jnp.float32
BF16 = jnp.bfloat16
LANES = 128
VMEM_LIMIT = 24 * 1024 * 1024
SMEM_SPEC = pl.BlockSpec(memory_space=pltpu.SMEM)
VMEM_SPEC = pl.BlockSpec(memory_space=pltpu.VMEM)


FLIP2 = [(0, 1), (1, 0)]
DIAGONAL = [(0, 3), (1, 2), (2, 1), (3, 0)]


def swap_half(array):
    return lax.ppermute(array, "l", FLIP2)


def after(value, *others):
    return lax.optimization_barrier((value, others))[0]


def split(value):
    high = value.astype(BF16)
    return high, (value - high.astype(F32)).astype(BF16)


def dot(a, b, dims):
    return lax.dot_general(a, b, (dims, ((), ())), preferred_element_type=F32)


NT = ((1,), (1,))
NN = ((1,), (0,))


def in_hbm(array):
    return pltpu.with_memory_space_constraint(array, pltpu.HBM)


def call(body, out_shape, hbm_outs=(), **kwargs):
    if hbm_outs:
        out_shape = [
            pltpu.HBM(a.shape, a.dtype) if i in hbm_outs else a for i, a in enumerate(out_shape)
        ]
    return pl.pallas_call(
        body,
        out_shape=out_shape,
        compiler_params=pltpu.CompilerParams(vmem_limit_bytes=VMEM_LIMIT),
        **kwargs,
    )


def cost(flops, byte_count):
    return pl.CostEstimate(flops=int(flops) // 64, bytes_accessed=int(byte_count) // 64, transcendentals=0)


def pack_body(frames, place_ref, in_ref, near_ref, far_ref, turned):
    slots = in_ref.shape[1]
    for start in range(0, slots, LANES):
        turned[start : start + LANES, :] = in_ref[:, start : start + LANES].T
    for rel in range(4):
        first = pl.multiple_of(place_ref[rel] * frames, 8)
        out = (near_ref, far_ref)[rel // 2]
        out[(rel % 2) * frames : (rel % 2 + 1) * frames, :] = turned[pl.ds(first, frames), :]


def pack(place, array, frames, waits=False):
    width, slots = array.shape
    out = jax.ShapeDtypeStruct((2 * frames, width), F32)
    return call(
        partial(pack_body, frames),
        grid=(1,),
        out_shape=[out, out],
        in_specs=[SMEM_SPEC, pl.BlockSpec((width, slots), lambda i: (0, 0))],
        out_specs=[pl.BlockSpec(out.shape, lambda i: (0, 0))] * 2,
        scratch_shapes=[pltpu.VMEM((slots, width), F32)],
        hbm_outs=(0, 1) if waits else (),
        cost_estimate=cost(0, 8 * width * slots),
        name="pack",
    )(place, in_hbm(array))


def part_spec(part, frames):
    array, i = part
    if i is None:
        return pl.BlockSpec(array.shape, lambda *_: (0,) * array.ndim)
    return pl.BlockSpec((frames, array.shape[1]), lambda *_: (i, 0))


def arrays_of(parts):
    return [array for array, _ in parts]


def unpack_body(frames, place_ref, *refs):
    ins, out_ref, turned = refs[:4], refs[4], refs[5]
    slots = out_ref.shape[1]
    for rel in range(4):
        first = pl.multiple_of(place_ref[rel] * frames, 8)
        turned[pl.ds(first, frames), :] = ins[rel][...]
    for start in range(0, slots, LANES):
        out_ref[:, start : start + LANES] = turned[start : start + LANES, :].T


def unpack(place, parts, frames, waited=False):
    width = parts[0][0].shape[1]
    slots = 4 * frames
    return call(
        partial(unpack_body, frames),
        grid=(1,),
        out_shape=jax.ShapeDtypeStruct((width, slots), F32),
        in_specs=[SMEM_SPEC] + [part_spec(part, frames) for part in parts],
        out_specs=pl.BlockSpec((width, slots), lambda i: (0, 0)),
        scratch_shapes=[pltpu.VMEM((slots, width), F32)],
        cost_estimate=cost(0, 8 * width * slots),
        name="unpack",
    )(place, *[in_hbm(a) if waited else a for a in arrays_of(parts)])


def merge_body(turn, kept_ref, come_ref, out_ref):
    frames, columns = kept_ref.shape
    width = columns // 2
    for i in range(2):
        some = slice((i ^ turn) * width, ((i ^ turn) + 1) * width)
        out_ref[i * frames : (i + 1) * frames, :] = kept_ref[:, some] + come_ref[:, some]


def merge(kept, half, come, turn=0):
    frames, columns = come.shape
    return call(
        partial(merge_body, turn),
        grid=(1,),
        out_shape=jax.ShapeDtypeStruct((2 * frames, columns // 2), F32),
        in_specs=[
            pl.BlockSpec((frames, columns), lambda i: (0, half)),
            pl.BlockSpec((frames, columns), lambda i: (0, 0)),
        ],
        out_specs=pl.BlockSpec((2 * frames, columns // 2), lambda i: (0, 0)),
        cost_estimate=cost(0, 12 * frames * columns),
        name="merge",
    )(kept, come)


def project_body(n_parts, n_flat, spots, n_weights, first, with_acc, with_stats, with_params, cols_ref, place_ref, *refs):
    del cols_ref

    def take(n):
        nonlocal refs
        some, refs = refs[:n], refs[n:]
        return some

    parts, flat_parts, weights = take(n_parts), take(n_flat), take(n_weights)
    acc, valid, stats_in, params = take(with_acc), take(with_stats > 0), take(with_stats > 1), take(with_params)
    (out_ref,) = take(1)
    stats, flat = take(with_stats > 0), take(n_flat > 0)
    x_high, x_low, far_ref = refs
    step = pl.program_id(0)
    width = x_high.shape[2]

    @pl.when(step == 0)
    def _():
        for block, part in zip(spots, parts):
            for start in range(0, part.shape[1], width):
                high, low = split(part[:, start : start + width])
                x_high[block + start // width] = high
                x_low[block + start // width] = low
        column = 0
        for part in flat_parts:
            flat[0][:, column : column + part.shape[1]] = part[...]
            column += part.shape[1]
        if with_acc:
            out_ref[...] = acc[0][...]
        else:
            out_ref[...] = jnp.zeros_like(out_ref)

    stacked = jnp.concatenate([x_high[step], x_low[step], x_high[step]], axis=1)
    for block, weight in enumerate(weight_blocks(place_ref, weights, far_ref)):
        w_high, w_low = split(weight)
        columns = slice(block * width, (block + 1) * width)
        out_ref[:, columns] += dot(stacked, jnp.concatenate([w_high, w_high, w_low], axis=1), NT)

    if with_stats:
        (stats_ref,) = stats

        @pl.when(step == pl.num_programs(0) - 1)
        def _():
            if stats_in:
                stats_ref[...] = stats_in[0][...]
            own = jnp.sum(valid[0][...], axis=0, keepdims=True)
            per = width // LANES
            for row in range(out_ref.shape[1] // LANES):
                z = out_ref[:, row * LANES : (row + 1) * LANES]
                total = jnp.sum(valid[0][...] * z, axis=0, keepdims=True)
                centred = valid[0][...] * (z - total / own)
                squares = jnp.sum(centred * centred, axis=0, keepdims=True)
                at = place_ref[first + row // per] * per + row % per
                stats_ref[0, pl.ds(at, 1), :] = total
                stats_ref[1, pl.ds(at, 1), :] = squares
                stats_ref[2, pl.ds(at, 1), :] = own
            if with_params:
                rest = params[0].shape[0] - 8
                stats_ref[3] = params[0][:8, :]
                stats_ref[4] = jnp.zeros_like(stats_ref[4])
                stats_ref[4, :rest, :] = params[0][8:, :]


def weight_specs(weights, layer, pairs=2):
    specs = []
    for weight in weights:
        if weight.ndim == 3:
            shape = (1, weight.shape[1], pairs * weight.shape[1])
            specs.append(pl.BlockSpec(shape, lambda s, cols, *_: (layer, 0, cols[s])))
        else:
            shape = (weight.shape[0], pairs * 4 * weight.shape[0])
            specs.append(pl.BlockSpec(shape, lambda s, cols, *_: (0, cols[s])))
    return specs


def far_scratch(width, pairs=2):
    return pltpu.VMEM((2, width, pairs * width), F32)


def weight_blocks(place_ref, refs, far_ref):
    near = [ref[0] for ref in refs if len(ref.shape) == 3]
    pieces = [ref for ref in refs if len(ref.shape) == 2]
    far = []
    for i in range(len(pieces) // 4):
        for rel, piece in enumerate(pieces[4 * i : 4 * i + 4]):
            rows = piece.shape[0]
            row = 2 * (place_ref[4] ^ (rel // 2)) + (place_ref[5] ^ (rel % 2))
            far_ref[i, pl.ds(pl.multiple_of(row * rows, rows), rows), :] = piece[...]
        far.append(far_ref[i])
    return near + far


def project(
    place, frames, parts, blocks, weights, layer, acc=None, valid=None, stats=None, params=None, flat=()
):
    near = weights[0].ndim == 3
    units = sum(1 if w.ndim == 3 else 0.25 for w in weights)
    width = weights[0].shape[1] if near else 4 * weights[0].shape[0]
    n = blocks.shape[0]
    spots, block = [], 0
    for array, _ in parts:
        spots.append(block)
        block += array.shape[1] // width
    full = pl.BlockSpec(memory_space=pltpu.VMEM)
    in_specs = [part_spec(part, frames) for part in (*parts, *flat)]
    in_specs += weight_specs(weights, layer, 1)
    operands = arrays_of(parts) + arrays_of(flat) + [in_hbm(w) for w in weights]
    array = jax.ShapeDtypeStruct((frames, int(units) * width), F32)
    array_spec = pl.BlockSpec(array.shape, lambda s, cols, place: (0, 0))
    out_shape, out_specs = [array], [array_spec]
    if acc is not None:
        in_specs.append(array_spec)
        operands.append(in_hbm(acc))
    if valid is not None:
        in_specs.append(full)
        operands.append(valid)
        shape = (3 if params is None else 5, 4 * width // LANES, LANES)
        out_shape.append(jax.ShapeDtypeStruct(shape, F32))
        out_specs.append(pl.BlockSpec(shape, lambda s, cols, place: (0, 0, 0)))
    for extra in (stats, params):
        if extra is not None:
            in_specs.append(full)
            operands.append(extra)
    if flat:
        out_shape.append(jax.ShapeDtypeStruct((frames, 4 * width), F32))
        out_specs.append(pl.BlockSpec((frames, 4 * width), lambda s, cols, place: (0, 0)))
    return call(
        partial(
            project_body,
            len(parts),
            len(flat),
            spots,
            len(weights),
            0 if near else 2,
            acc is not None,
            (valid is not None) + (stats is not None),
            params is not None,
        ),
        grid_spec=pltpu.PrefetchScalarGridSpec(
            num_scalar_prefetch=2,
            grid=(n,),
            in_specs=in_specs,
            out_specs=out_specs,
            scratch_shapes=[pltpu.VMEM((n, frames, width), BF16)] * 2 + [far_scratch(width, 1)],
        ),
        out_shape=out_shape,
        hbm_outs=(0, len(out_shape) - 1) if flat else (0,),
        cost_estimate=cost(6 * frames * n * width * units * width, 4 * n * width * units * width),
        name="project",
    )(blocks, place, *operands)


def to_relative(place_ref, spread, rows_ref, value, slot):
    per = value.shape[0] // 4
    spread[...] = value
    for rel in range(4):
        first = place_ref[rel] * per
        for row in range(per):
            rows_ref[slot, rel * per + row : rel * per + row + 1, :] = spread[
                pl.ds(first + row, 1), :
            ]


def tree(values):
    while len(values) > 1:
        values = [a + b for a, b in zip(values[::2], values[1::2])]
    return values[0]


def gathered(ref, slot):
    return [ref[i] for i in range(slot, ref.shape[0], ref.shape[0] // 16)]


def norm_terms(stats_ref):
    each = [gathered(stats_ref, slot) for slot in range(3)]
    totals, squares, owns = each
    count = tree(owns)
    mean = tree(totals) / count
    away = [total / own - mean for total, own in zip(totals, owns)]
    spread = tree([s + n * a * a for s, n, a in zip(squares, owns, away)])
    return count, mean, lax.rsqrt(spread / count + EPS)


CHUNKS = 4


def columns_of(refs, row):
    for ref in refs:
        if row * LANES < ref.shape[1]:
            return ref[:, row * LANES : (row + 1) * LANES]
        row -= ref.shape[1] // LANES


def recur_body(n_z, last, layer, spread_params, place_ref, gate_ref, *refs):
    z_refs, refs = refs[:n_z], refs[n_z:]
    (stats_ref, params_ref, valid_ref, x_ref), refs = refs[:4], refs[4:]
    outs, refs = refs[: 1 + 3 * last], refs[1 + 3 * last :]
    if spread_params:
        state_ref, slope_ref, params_out, rows, spread, held, drive_s, state_s, slope_s = refs
    else:
        state_ref, slope_ref, rows, spread, held, drive_s, state_s, slope_s = refs
    frames, features = x_ref.shape
    blocks = features // LANES
    per = blocks // 4
    chunk = pl.program_id(0)

    @pl.when(chunk == 0)
    def _():
        if spread_params:
            for rel in range(4):
                first = place_ref[rel] * (stats_ref.shape[0] // 16) + 3
                for row in range(LAYERS * 3 * per):
                    at = rel * per + row % per
                    params_out[row // per, at : at + 1, :] = stats_ref[
                        first + row // 8, row % 8 : row % 8 + 1, :
                    ]
            params = [params_out[3 * layer + i] for i in range(3)]
        else:
            params = [params_ref[3 * layer + i] for i in range(3)]
        _, mean, inv_std = norm_terms(stats_ref)
        to_relative(place_ref, spread, rows, mean, 0)
        to_relative(place_ref, spread, rows, inv_std, 1)
        rows[1] = rows[1] * params[0]
        rows[2] = params[1]
        rows[3] = params[2]
        held[...] = jnp.zeros_like(held)

    for row in range(blocks):
        drive_s[row * frames : (row + 1) * frames, :] = (
            columns_of(z_refs, row) - rows[0, row : row + 1, :]
        ) * rows[1, row : row + 1, :] + rows[2, row : row + 1, :]
    decay = rows[3]

    def step(t, state):
        at = pl.ds(t, blocks, stride=frames)
        pre = drive_s[at, :] + decay * state
        half = 0.5 + 0.5 * lax.erf(pre * (1.0 / ROOT_TWO))
        gate = gate_ref[chunk * frames + t] > 0.0
        slope = half + pre * jnp.exp(-0.5 * pre * pre) * (1.0 / ROOT_TWO_PI)
        state = jnp.where(gate, pre * half, state)
        state_s[at, :] = state
        slope_s[at, :] = jnp.where(gate, slope, 0.0)
        return state

    held[...] = lax.fori_loop(0, frames, step, held[...], unroll=8)
    valid = valid_ref[...]
    for row in range(blocks):
        lanes = slice(row * LANES, (row + 1) * LANES)
        state = state_s[row * frames : (row + 1) * frames, :]
        state_ref[:, lanes] = state
        slope_ref[:, lanes] = slope_s[row * frames : (row + 1) * frames, :]
        value = x_ref[:, lanes] + valid * state
        out, at = (outs[row // per], row % per) if last else (outs[0], row)
        out[:, at * LANES : (at + 1) * LANES] = value


def recur(layer, place, gate, z, stats, params, valid, x, last):
    frames, features = x.shape
    blocks = features // LANES
    some = frames // CHUNKS
    whole = lambda array: pl.BlockSpec(array.shape, lambda i: (0,) * array.ndim)
    by_chunk = lambda array: pl.BlockSpec((some, array.shape[1]), lambda i: (i, 0))
    full = jax.ShapeDtypeStruct((frames, features), F32)
    piece = jax.ShapeDtypeStruct((frames, features // 4), F32)
    out_shape = [piece] * 4 if last else [full]
    out_shape += [full, full]
    out_specs = [by_chunk(a) for a in out_shape]
    spread_params = params is None
    if spread_params:
        out_shape.append(jax.ShapeDtypeStruct((3 * LAYERS, blocks, LANES), F32))
        out_specs.append(whole(out_shape[-1]))
        params = valid
    return call(
        partial(recur_body, len(z), last, layer, spread_params),
        grid=(CHUNKS,),
        in_specs=[SMEM_SPEC, SMEM_SPEC]
        + [by_chunk(a) for a in z]
        + [whole(a) for a in (stats, params)]
        + [by_chunk(a) for a in (valid, x)],
        out_specs=out_specs,
        out_shape=out_shape,
        hbm_outs=tuple(range(len(out_shape) - spread_params)) if last else (1, 2),
        scratch_shapes=[
            pltpu.VMEM((4, blocks, LANES), F32),
            pltpu.VMEM((blocks, LANES), F32),
            pltpu.VMEM((blocks, LANES), F32),
        ]
        + [pltpu.VMEM((blocks * some, LANES), F32)] * 3,
        cost_estimate=cost(100 * frames * features, 20 * frames * features),
        name="recur",
    )(place, gate, *[in_hbm(a) for a in z], stats, params, valid, in_hbm(x))


def back_body(n_z, n_ups, spots, layer, place_ref, gate_ref, *refs):
    z_refs, refs = refs[:n_z], refs[n_z:]
    (stats_ref, params_ref), refs = refs[:2], refs[2:]
    ups, (state_ref, slope_ref), refs = refs[:n_ups], refs[n_ups : n_ups + 2], refs[n_ups + 2 :]
    grad_ref, sums_ref, rows, spread, held, up_s, state_s, slope_s = refs
    frames, features = state_ref.shape
    blocks = features // LANES
    per = blocks // 4
    tall = frames + 8
    step_no = pl.program_id(0)
    chunk = pl.num_programs(0) - 1 - step_no

    @pl.when(step_no == 0)
    def _():
        _, mean, inv_std = norm_terms(stats_ref)
        to_relative(place_ref, spread, rows, mean, 0)
        to_relative(place_ref, spread, rows, inv_std, 1)
        held[...] = jnp.zeros_like(held)

    for row in range(blocks):
        lanes = slice(row * LANES, (row + 1) * LANES)
        base = row * frames
        up = None
        for (_, column), part in zip(spots, ups):
            if column <= row * LANES < column + part.shape[1]:
                value = part[:, row * LANES - column : (row + 1) * LANES - column]
                up = value if up is None else up + value
        up_s[base : base + frames, :] = up
        state_s[row * tall : row * tall + 8, :] = jnp.zeros((8, LANES), F32)
        state_s[row * tall + 8 : (row + 1) * tall, :] = state_ref[:, lanes]
        slope_s[base : base + frames, :] = slope_ref[:, lanes]
    decay = params_ref[3 * layer + 2]

    def step(i, carry):
        t = frames - 1 - i
        at = pl.ds(t, blocks, stride=frames)
        slope = slope_s[at, :]
        gate = gate_ref[chunk * frames + t]
        total = gate * up_s[at, :] + carry
        up_s[at, :] = total * slope
        return total * (slope * decay + (1.0 - gate))

    held[0] = lax.fori_loop(0, frames, step, held[0], unroll=8)
    held[4] += held[1] * state_s[pl.ds(tall - 1, blocks, stride=tall), :]
    held[1] = up_s[pl.ds(0, blocks, stride=frames), :]
    for row in range(blocks):
        lanes = slice(row * LANES, (row + 1) * LANES)
        grad = up_s[row * frames : (row + 1) * frames, :]
        grad_ref[:, lanes] = grad
        zhat = (columns_of(z_refs, row) - rows[0, row : row + 1, :]) * rows[1, row : row + 1, :]
        before = state_s[row * tall + 7 : row * tall + 7 + frames, :]
        for slot, value in enumerate((grad * zhat, grad, grad * before)):
            held[2 + slot, row : row + 1, :] += jnp.sum(value, axis=0, keepdims=True)

    @pl.when(chunk == 0)
    def _():
        for row in range(blocks):
            at = place_ref[row // per] * per + row % per
            for slot in range(3):
                sums_ref[slot, pl.ds(at, 1), :] = held[2 + slot, row : row + 1, :]


def spots_of_sum(parts, width):
    spots, column = [], 0
    for array, _ in parts:
        spots.append((0, column % (4 * width)))
        column += array.shape[1]
    return spots


def back(layer, place, gate, z, stats, params, ups, states, slopes):
    frames, features = states.shape
    width = features // 4
    blocks = features // LANES
    some = frames // CHUNKS
    whole = lambda array: pl.BlockSpec(array.shape, lambda i: (0,) * array.ndim)

    def by_chunk(array, first=0):
        return pl.BlockSpec(
            (some, array.shape[1]), lambda i: ((first or 0) * CHUNKS + CHUNKS - 1 - i, 0)
        )

    out_shape = [
        jax.ShapeDtypeStruct((frames, features), F32),
        jax.ShapeDtypeStruct((3, blocks, LANES), F32),
    ]
    return call(
        partial(back_body, len(z), len(ups), spots_of_sum(ups, width), layer),
        grid=(CHUNKS,),
        in_specs=[SMEM_SPEC] * 2
        + [by_chunk(a) for a in z]
        + [whole(a) for a in (stats, params)]
        + [by_chunk(*up) for up in ups]
        + [by_chunk(a) for a in (states, slopes)],
        out_specs=[by_chunk(out_shape[0]), whole(out_shape[1])],
        out_shape=out_shape,
        scratch_shapes=[
            pltpu.VMEM((2, blocks, LANES), F32),
            pltpu.VMEM((blocks, LANES), F32),
            pltpu.VMEM((5, blocks, LANES), F32),
            pltpu.VMEM((blocks * some, LANES), F32),
            pltpu.VMEM((blocks * (some + 8), LANES), F32),
            pltpu.VMEM((blocks * some, LANES), F32),
        ],
        cost_estimate=cost(30 * frames * features, 20 * frames * features),
        name="back",
    )(
        place,
        gate,
        *[in_hbm(a) for a in z],
        stats,
        params,
        *arrays_of(ups),
        in_hbm(states),
        in_hbm(slopes),
    )


def input_terms(high_s, low_s, weights):
    left, right = [], []
    for block, weight in enumerate(weights):
        w_high, w_low = split(weight)
        left += [high_s[block], low_s[block], high_s[block]]
        right += [w_high, w_high, w_low]
    return dot(jnp.concatenate(left, axis=1), jnp.concatenate(right, axis=0), NN)


def norm_back_body(n_z, split_terms, layer, cols_ref, place_ref, grad_ref, *refs):
    del cols_ref
    z_refs, refs = refs[:n_z], refs[n_z:]
    params_ref, valid_ref, stats_ref, sums_ref, *refs = refs
    weights, refs = refs[:10], refs[10:]
    if split_terms:
        out_ref, leave_ref, near_term_ref, far_term_ref, sums_out_ref, *refs = refs
        term_refs, starts = (far_term_ref, near_term_ref), (0, 0)
    else:
        out_ref, leave_ref, term_ref, sums_out_ref, *refs = refs
        term_refs, starts = (term_ref, term_ref), (2 * grad_ref.shape[1] // 4, 0)
    rows, spread, high_s, low_s, far_ref = refs
    blocks = grad_ref.shape[1] // LANES
    width = high_s.shape[2]
    per = width // LANES

    @pl.when(pl.program_id(0) == 0)
    def _():
        count, mean, inv_std = norm_terms(stats_ref)
        to_relative(place_ref, spread, rows, mean, 0)
        to_relative(place_ref, spread, rows, inv_std, 1)
        rows[2] = rows[1] * params_ref[3 * layer]
        sums = [tree(gathered(sums_ref, slot)) for slot in range(3)]
        for slot in range(3):
            sums_out_ref[slot] = sums[slot]
        to_relative(place_ref, spread, rows, sums[0] / count, 3)
        to_relative(place_ref, spread, rows, sums[1] / count, 4)
        valid = valid_ref[...]
        for row in range(blocks):
            lanes = slice(row * LANES, (row + 1) * LANES)
            one = lambda slot: rows[slot, row : row + 1, :]
            zhat = (columns_of(z_refs, row) - one(0)) * one(1)
            value = one(2) * (grad_ref[:, lanes] - valid * (one(4) + zhat * one(3)))
            out_ref[:, lanes] = value
            if (row // per) % 2:
                at = (row // per // 2) * width + (row % per) * LANES
                leave_ref[:, at : at + LANES] = value
            high, low = split(value)
            inner = slice((row % per) * LANES, (row % per + 1) * LANES)
            high_s[row // per, :, inner] = high
            low_s[row // per, :, inner] = low

    value = input_terms(high_s, low_s, weight_blocks(place_ref, weights, far_ref))
    for step, (term_ref, first) in enumerate(zip(term_refs, starts)):

        @pl.when(pl.program_id(0) == step)
        def _():
            for pair in range(2):
                at = pl.multiple_of(((place_ref[0] & 1) ^ pair) * width, width)
                term_ref[:, pl.ds(first + at, width)] = value[
                    :, pair * width : (pair + 1) * width
                ]


def norm_back(columns, place, grad, z, params, valid, stats, sums, weights, layer, split_terms):
    frames, features = grad.shape
    width = features // 4
    blocks = features // LANES
    whole = lambda array: pl.BlockSpec(array.shape, lambda s, cols, place: (0,) * array.ndim)
    operands = [grad, *[in_hbm(a) for a in z], params, valid, stats, sums]
    full = jax.ShapeDtypeStruct((frames, features), F32)
    half = jax.ShapeDtypeStruct((frames, 2 * width), F32)
    terms = [half, half] if split_terms else [full]
    out_shape = [full, half, *terms, jax.ShapeDtypeStruct((3, blocks, LANES), F32)]
    return call(
        partial(norm_back_body, len(z), split_terms, layer),
        grid_spec=pltpu.PrefetchScalarGridSpec(
            num_scalar_prefetch=2,
            grid=(2,),
            in_specs=[whole(a) for a in operands] + weight_specs(weights, layer),
            out_specs=[whole(a) for a in out_shape],
            scratch_shapes=[
                pltpu.VMEM((5, blocks, LANES), F32),
                pltpu.VMEM((blocks, LANES), F32),
                pltpu.VMEM((4, frames, width), BF16),
                pltpu.VMEM((4, frames, width), BF16),
                far_scratch(width),
            ],
        ),
        out_shape=out_shape,
        hbm_outs=(0,),
        cost_estimate=cost(6 * frames * features * features, 4 * features * features),
        name="norm_back",
    )(columns, place, *operands, *[in_hbm(w) for w in weights])


def own_terms_body(n_ups, spots, cols_ref, place_ref, grad_ref, *refs):
    del cols_ref
    ups, refs = refs[:n_ups], refs[n_ups:]
    weights, refs = refs[:10], refs[10:]
    out_ref, high_s, low_s, far_ref = refs
    width = high_s.shape[2]
    step = pl.program_id(0)

    @pl.when(step == 0)
    def _():
        for block in range(4):
            high, low = split(grad_ref[:, block * width : (block + 1) * width])
            high_s[block] = high
            low_s[block] = low

    value = input_terms(high_s, low_s, weight_blocks(place_ref, weights, far_ref))
    for pair in range(2):
        at = pl.multiple_of(((place_ref[0] & 1) ^ pair) * width, width)
        out_ref[:, pl.ds(at, width)] = value[:, pair * width : (pair + 1) * width]
    for half in range(2):

        @pl.when(step == half)
        def _():
            first = 2 * half * width
            for (_, column), up in zip(spots, ups):
                low = max(column, first)
                high = min(column + up.shape[1], first + 2 * width)
                if low < high:
                    out_ref[:, low - first : high - first] += up[:, low - column : high - column]


def own_terms(columns, place, grad, ups, weights, layer):
    frames, features = grad.shape
    width = features // 4
    whole = lambda array: pl.BlockSpec(array.shape, lambda s, cols, place: (0,) * array.ndim)
    step_block = pl.BlockSpec((frames, 2 * width), lambda s, cols, place: (0, s))
    return call(
        partial(own_terms_body, len(ups), spots_of_sum(ups, width)),
        grid_spec=pltpu.PrefetchScalarGridSpec(
            num_scalar_prefetch=2,
            grid=(2,),
            in_specs=[whole(grad)]
            + [part_spec(up, frames) for up in ups]
            + weight_specs(weights, layer),
            out_specs=step_block,
            scratch_shapes=[pltpu.VMEM((4, frames, width), BF16)] * 2 + [far_scratch(width)],
        ),
        out_shape=jax.ShapeDtypeStruct((frames, features), F32),
        cost_estimate=cost(6 * frames * features * features, 4 * features * features),
        name="own_terms",
    )(columns, place, in_hbm(grad), *arrays_of(ups), *[in_hbm(w) for w in weights])


def prepare_body(lists_ref, place_ref, own_ref, near_ref, high_ref, low_ref):
    del lists_ref
    padded = high_ref.shape[0] // 2
    width = high_ref.shape[1] // 2
    for clip, part in enumerate((own_ref, near_ref)):
        rows = part.shape[0]
        for dc in range(2):
            at = pl.multiple_of((place_ref[6] ^ clip ^ dc) * width, width)
            high, low = split(part[:, dc * width : (dc + 1) * width])
            high_ref[clip * padded : clip * padded + rows, pl.ds(at, width)] = high
            low_ref[clip * padded : clip * padded + rows, pl.ds(at, width)] = low
        zeros = jnp.zeros((padded - rows, 2 * width), BF16)
        high_ref[clip * padded + rows : (clip + 1) * padded, :] = zeros
        low_ref[clip * padded + rows : (clip + 1) * padded, :] = zeros


def prepare(place, own, near):
    frames, features = own.shape
    width = features // 4
    padded = -(-frames // LANES) * LANES
    in_spec = pl.BlockSpec((frames, 2 * width), lambda s, *_: (0, s))
    out = jax.ShapeDtypeStruct((2 * padded, features), BF16)
    out_spec = pl.BlockSpec((2 * padded, 2 * width), lambda s, order, place: (0, order[s]))
    order = jnp.stack([place[0] >> 1, 1 - (place[0] >> 1)])
    return call(
        prepare_body,
        grid_spec=pltpu.PrefetchScalarGridSpec(
            num_scalar_prefetch=2,
            grid=(2,),
            in_specs=[in_spec, in_spec],
            out_specs=[out_spec, out_spec],
        ),
        out_shape=[out, out],
        hbm_outs=(0, 1),
        cost_estimate=cost(0, 16 * frames * features),
        name="prepare",
    )(order, place, in_hbm(own), in_hbm(near))


def product(g_high, g_low, x_high, x_low):
    return dot(g_high, x_high, NN) + (dot(g_high, x_low, NN) + dot(g_low, x_high, NN))


def weight_body(turn, place_ref, *refs):
    if turn:
        grad_ref, near_ref, x_high, x_low, kept, sent, g_high, g_low, t_high, t_low = refs

        @pl.when(pl.program_id(0) == 0)
        def _():
            frames, features = grad_ref.shape
            width = features // 4
            rows = width // 4
            padded = t_high.shape[1] // 2
            t_high[...] = jnp.zeros_like(t_high)
            t_low[...] = jnp.zeros_like(t_low)
            for clip in range(2):
                for dh in range(2):
                    if clip == 0:
                        part = grad_ref[:, 2 * dh * width : (2 * dh + 1) * width]
                    else:
                        part = near_ref[:, dh * width : (dh + 1) * width]
                    high, low = split(part.T)
                    at = (
                        slice(dh * width, (dh + 1) * width),
                        slice(clip * padded, clip * padded + frames),
                    )
                    t_high[at] = high
                    t_low[at] = low
            for group in range(8):
                first, second, dh = group // 4, group // 2 % 2, group % 2
                core = place_ref[6]
                y = place_ref[4] ^ (first * core + second * (1 - core))
                x = place_ref[5] ^ (first * (1 - core) + second * core)
                at = pl.multiple_of(dh * width + (2 * y + x) * rows, rows)
                g_high[group * rows : (group + 1) * rows, :] = t_high[pl.ds(at, rows), :]
                g_low[group * rows : (group + 1) * rows, :] = t_low[pl.ds(at, rows), :]

    else:
        g_high, g_low, x_high, x_low, kept, sent = refs
    half = g_high.shape[0] // 2
    value = product(g_high[...], g_low[...], x_high[...], x_low[...])
    kept[...] = value[:half].reshape(kept.shape)
    sent[...] = value[half:].reshape(sent.shape)


def weight_rows(side, place, grads, x_split, width):
    turn = side == 0
    whole = lambda array: pl.BlockSpec(array.shape, lambda s, place: (0,) * array.ndim)
    x_spec = pl.BlockSpec((x_split[0].shape[0], width), lambda s, place: (0, s))
    shape = (2, 2, width // 4, 4 * width)
    out_shape = [jax.ShapeDtypeStruct(shape, F32)] * 2
    out_specs = [pl.BlockSpec(shape[:3] + (width,), lambda s, place: (0, 0, 0, s))] * 2
    scratch = []
    if turn:
        turned = (2 * width, x_split[0].shape[0])
        out_shape += [jax.ShapeDtypeStruct(turned, BF16)] * 2
        out_specs += [whole(out_shape[-1])] * 2
        scratch = [pltpu.VMEM(turned, BF16)] * 2
    return call(
        partial(weight_body, turn),
        grid_spec=pltpu.PrefetchScalarGridSpec(
            num_scalar_prefetch=1,
            grid=(4,),
            in_specs=[whole(a) for a in grads] + [x_spec] * 2,
            out_specs=out_specs,
            scratch_shapes=scratch,
        ),
        out_shape=out_shape,
        hbm_outs=(0,),
        cost_estimate=cost(12 * x_split[0].shape[0] * width * 4 * width, 4 * 8 * width * width),
        name="weight_rows",
    )(place, *([in_hbm(grads[0]), grads[1]] if turn else grads), *[in_hbm(x) for x in x_split])


def step_body(n, widths, cut, *refs):
    ins, outs = refs[: 2 * n], refs[2 * n :]
    starts = [sum(widths[:i]) for i in range(len(widths))]
    column = 0
    for i in range(n):
        total = ins[2 * i][...] + ins[2 * i + 1][...]
        end = column + total.shape[-1]
        for j, (start, columns) in enumerate(zip(starts, widths)):
            low, high = max(start, column), min(start + columns, end)
            if low < high:
                to = (Ellipsis, slice(low - start, high - start))
                piece = total[..., low - column : high - column]
                pieces = [piece]
                for _ in range(cut):
                    pieces = [half[k] for half in pieces for k in range(2)]
                for k, some in enumerate(pieces):
                    outs[len(pieces) * j + k][to] = some
        column = end


def step_of(*pairs, cut=1, widths=None):
    shape = list(pairs[0][0].shape)
    widths = widths or [sum(pair[0].shape[-1] for pair in pairs)]
    outs = []
    for columns in widths:
        shape[-1] = columns
        outs += [jax.ShapeDtypeStruct(tuple(shape[cut:]), F32)] * 2**cut
    whole = lambda array: pl.BlockSpec(array.shape, lambda i: (0,) * array.ndim)
    operands = [array for pair in pairs for array in pair]
    return call(
        partial(step_body, len(pairs), widths, cut),
        grid=(1,),
        in_specs=[whole(a) for a in operands],
        out_specs=[whole(a) for a in outs],
        out_shape=outs,
        cost_estimate=cost(0, 4 * sum(a.size for a in operands)),
        name="reduction_step",
    )(*operands)


def plane_swap(array, step):
    pairs = []
    for i in range(8):
        over_x = (i % 2 == 0) == (step == 0)
        pairs.append((i, i ^ 2 if over_x else i ^ 4))
    return lax.ppermute(array, ("y", "x", "c"), pairs)


def plane_gather(share, *before):
    first = plane_swap(share, 0)
    second = plane_swap(share, 1)
    return [share, second, first, plane_swap(after(first, second, *before), 1)]


def assemble_body(by_core, place_ref, *refs):
    out_ref = refs[-1]
    core = place_ref[6] if by_core else 1
    rows, columns = refs[0].shape
    quarter = columns // 4
    for i in range(4):
        first, second = i // 2, i % 2
        y = place_ref[4] ^ (first * core + second * (1 - core))
        x = place_ref[5] ^ (first * (1 - core) + second * core)
        at = pl.multiple_of((2 * y + x) * rows, rows)
        for side in range(2):
            for h in range(2):
                to = pl.multiple_of((2 * h + (place_ref[7] ^ side)) * quarter, quarter)
                some = slice((2 * side + h) * quarter, (2 * side + h + 1) * quarter)
                out_ref[0, pl.ds(at, rows), pl.ds(to, quarter)] = refs[i][:, some]


def assemble(place, pieces, layer, onto=None, by_core=True):
    rows, columns = 4 * pieces[0].shape[0], pieces[0].shape[1]
    aliases, extra, extra_specs = {}, [], []
    if onto is not None:
        aliases, extra = {1 + len(pieces): 0}, [onto]
        extra_specs = [pl.BlockSpec(memory_space=pl.ANY)]
    (out,) = call(
        partial(assemble_body, by_core),
        grid=(1,),
        out_shape=[jax.ShapeDtypeStruct((LAYERS, rows, columns), F32)],
        hbm_outs=(0,),
        in_specs=[SMEM_SPEC]
        + [pl.BlockSpec(p.shape, lambda i: (0, 0)) for p in pieces]
        + extra_specs,
        out_specs=[pl.BlockSpec((1, rows, columns), lambda i: (layer, 0, 0))],
        input_output_aliases=aliases,
        cost_estimate=cost(0, 8 * rows * columns),
        name="assemble",
    )(place, *[p if extra else in_hbm(p) for p in pieces], *extra)
    return out


def half_features(inputs, weights, gains, shifts, decays, biases, lengths, frame_mask, grad_out):
    width, slots = inputs.shape
    clips, frames = frame_mask.shape
    depth = weights.shape[2]
    blocks = 4 * width // LANES
    y, x, h, l, c = (lax.axis_index(name) for name in ("y", "x", "h", "l", "c"))
    b = 2 * y + x
    numbers = [2 * (h ^ (rel // 2)) + (c ^ (rel % 2)) for rel in range(4)] + [y, x, c, l]
    place = jnp.stack(numbers).astype(jnp.int32)
    own_blocks, other_blocks = (
        jnp.stack(
            [2 * (2 * (h ^ (rel // 2)) + half) + (c ^ (rel % 2)) for rel in range(4)]
        ).astype(jnp.int32)
        for half in (l, 1 - l)
    )
    own_columns = jnp.stack([2 * h + l, 2 * (1 - h) + l]).astype(jnp.int32)
    other_columns = jnp.stack([2 * (1 - h) + 1 - l, 2 * h + 1 - l]).astype(jnp.int32)
    rows = width // 4

    clip = 2 * h + c
    seen = lax.dynamic_index_in_dim(frame_mask, clip, 0, keepdims=False)
    length = lax.dynamic_index_in_dim(lengths, clip, 0, keepdims=False)
    moments = jnp.arange(frames, dtype=jnp.int32)
    gate = ((moments < length) & ((seen == 1) | (moments == 0))).astype(F32)
    valid = jnp.broadcast_to(gate[:, None], (frames, LANES))

    def far_share(layer):
        return lax.dynamic_slice(weights, (layer, b * rows, 0), (1, rows, depth))[0]

    def over_h(array):
        return lax.ppermute(array, "h", FLIP2)

    def over_c(array):
        return lax.ppermute(array, "c", FLIP2)

    def over_second(array):
        return plane_swap(array, 1)

    def four_of(near_rows, far_rows):
        return [
            (near_rows, 0),
            (over_c(near_rows), 1),
            (far_rows, 0),
            (over_c(far_rows), 1),
        ]

    def four_of_plane(share):
        both = lax.ppermute(share, ("y", "x"), DIAGONAL)
        return [share, lax.ppermute(share, "x", FLIP2), lax.ppermute(share, "y", FLIP2), both]

    near = over_c(weights)
    share = far_share(0)
    close, away = pack(place, after(inputs, share), frames)
    share = over_h(share)
    away = over_h(away)
    other_close = swap_half(close)
    up_close, up_away = pack(place, after(grad_out, close), frames, waits=True)
    share = after(share, up_close, valid, near, other_close)
    pieces = four_of_plane(share)
    away = after(away, pieces[1:])
    half_weights = [[weights, near, *pieces, *map(over_c, after(pieces, away))]]
    own = four_of(after(close, away), away)
    other_away = swap_half(away)
    others = [(other_close, 0), (over_c(other_close), 1)]
    params = jnp.stack([gains, shifts + biases, decays], axis=1)
    own_params = params.reshape(LAYERS * 3 * width // LANES, LANES)
    params = None

    def gather(array, axes):
        return lax.all_gather(array, axes, tiled=True)

    weight = half_weights[0]
    early = jnp.concatenate([own_blocks, other_blocks[:2]])
    z, own_flat = project(place, frames, own + others, early, weight, 0, flat=own)
    others += [(other_away, 0), (over_c(after(other_away, z)), 1)]
    z, stats, other_flat = project(
        place,
        frames,
        others[2:],
        other_blocks[2:],
        weight,
        0,
        z,
        valid,
        params=own_params,
        flat=others,
    )
    z = [z]
    stats = gather(stats, ("h", "c"))
    share = over_c(lax.ppermute(after(far_share(1), stats), ("h", "c"), DIAGONAL))
    stats = gather(stats, ("y", "x"))
    x, states, slopes, params = recur(0, place, gate, z, stats, None, valid, own_flat, False)
    own_near, other_near = over_c(after(own_flat, z[0])), over_c(after(other_flat, z[0]))
    x_near = over_c(x)
    own_split = prepare(place, after(own_flat, x_near), own_near)
    other_split = prepare(place, after(other_flat, x_near), other_near)
    saved = [(own_split, other_split, z, stats, states, slopes)]

    pieces = four_of_plane(after(share, slopes, own_near, other_near))
    near = [weights, near]
    other = swap_half(x)
    x_own = after(x, own_split[0], other_split[0])
    z, *_ = project(place, frames, [(x_own, None)], own_blocks, near, 1)
    own_split = prepare(place, after(x, z), x_near)
    far = [*pieces, *map(over_c, after(pieces, own_split[0]))]
    up_away = over_h(after(up_away, other, own_split[0]))
    half_weights.append(near + far)
    z, stats = project(place, frames, [(other, None)], other_blocks, near, 1, z, valid)
    both = jnp.concatenate([own_blocks, other_blocks])
    z_far, stats = project(
        place,
        frames,
        [(x, None), (other, None)],
        both,
        far,
        1,
        None,
        valid,
        stats,
    )
    z = [z, z_far]
    stats = gather(gather(stats, ("y", "x")), ("h", "c"))
    upstream = four_of(up_close, after(up_away, stats))
    *output, states, slopes = recur(1, place, gate, z, stats, params, valid, x, True)
    other_near = over_c(after(other, slopes))
    saved.append((own_split, (other, other_near), z, stats, states, slopes))
    diagonal = over_c(over_h(output[3]))

    ups = upstream
    results = [None] * LAYERS
    for layer in range(LAYERS - 1, -1, -1):
        own_split, other_split, z, stats, states, slopes = saved[layer]
        weight = half_weights[layer]
        grad_pre, sums = back(layer, place, gate, z, stats, params, ups, states, slopes)
        sums = gather(sums, ("y", "x"))
        if layer == 0:
            come[0] = after(come[0], sums, away)
            later, go = step_of((in_hbm(stay[0]), come[0]), (in_hbm(stay[1]), come[1]))
            sums = after(sums, later)
            go = over_second(go)
        sums = gather(sums, ("h", "c"))
        grad_z, leaving, *terms, sums = norm_back(
            other_columns, place, grad_pre, z, params, valid, stats, sums, weight, layer,
            layer == 0,
        )
        leaving = over_c(leaving)
        if layer > 0:
            received = [swap_half(terms[0])]
            other_split = prepare(place, *after(other_split, grad_z))
            leaving = after(leaving, diagonal, other_split[0])
        else:
            received = [None, swap_half(terms[1])]
            later, go = step_of((later, after(go, grad_z)))
            leaving = after(leaving, later)
            go = lax.ppermute(go, ("h", "c"), DIAGONAL)
            later = (later, go)
        *first, g_high, g_low = weight_rows(0, place, (grad_z, leaving), own_split, width)
        turned = (g_high, g_low)
        come = [plane_swap(first[1], 0)]
        if layer == 0:
            received[0] = swap_half(after(terms[0], received[1]))
        second = weight_rows(1, place, turned, other_split, width)
        if layer > 0:
            away = over_h(after(output[2], second[0]))
            output = [(a, 0) for a in (output[0], over_c(output[1]), away, diagonal)]
        come.append(plane_swap(second[1], 0))
        stay = (first[0], second[0])
        kept = own_terms(own_columns, place, after(grad_z, second[0]), ups, weight, layer)
        ups = [(kept, None)] + [(r, None) for r in received]
        results[layer] = lax.dynamic_index_in_dim(
            sums.reshape(3, 4, width), clip, axis=1, keepdims=False
        )

    sums = jnp.stack(results)
    sums = [sums[:, 0], sums[:, 1], sums[:, 2]]
    away = merge(kept, 1, received[1], turn=1)
    later = (later[0], over_c(after(later[1], away)))
    come[0] = after(come[0], sums, later[1], output[1][0])
    away = over_h(away)
    near_sum, far_sum, near_go, far_go = step_of(
        (in_hbm(stay[0]), come[0]), (in_hbm(stay[1]), come[1]), cut=2
    )
    near_go, far_go = over_second(near_go), over_second(far_go)
    (go,) = step_of((far_sum, far_go), cut=0)
    (later,) = step_of(later, cut=0)
    later = four_of_plane(after(later, go, near_go))
    go = over_h(go)
    (total,) = step_of((near_sum, near_go), cut=0)
    output = unpack(place, [(after(array, total), i) for array, i in output], frames, waited=True)
    close = merge(kept, 0, after(received[0], output))
    far = over_c(after(away, received[0])[: 3 * frames // 2])
    (share,) = step_of((total, after(go, far, close, *later[1:])), cut=0)
    grad_in = [(close, 0), (over_c(close[frames:]), 0), (away, 1), (far, 0)]
    grad_in = unpack(place, grad_in, frames)
    grad_weights = assemble(place, after(later, grad_in), 1, by_core=False)
    gathered = plane_gather(share, grad_weights)
    grad_weights = assemble(place, gathered, 0, grad_weights)
    return (output, grad_in, grad_weights, *sums, sums[1])


def gelu_slope(value):
    return (
        0.5 * (1.0 + jax.scipy.special.erf(value / ROOT_TWO))
        + value * jnp.exp(-0.5 * value * value) / ROOT_TWO_PI
    )


def recur_step(decay, state, inputs):
    drive_t, valid_t = inputs
    pre = drive_t + decay * state
    state = state + valid_t * (jax.nn.gelu(pre, approximate=False) - state)
    return (state, state)


def back_step(decay, carry, inputs):
    upstream_t, valid_t, pre_t = inputs
    total = upstream_t + carry
    grad_pre = total * valid_t * gelu_slope(pre_t)
    carry = total * (1.0 - valid_t) + grad_pre * decay
    return (carry, grad_pre)


def add_piece(weight, piece):
    return jnp.dot(weight, piece, precision=HIGH, preferred_element_type=jnp.float32)


def weight_columns(grad_pre_norm, piece):
    return jnp.einsum("jf,kf->jk", grad_pre_norm, piece, precision=HIGH)


def split_features(inputs, weights, gains, shifts, decays, biases, lengths, frame_mask, grad_out):
    width, slots = inputs.shape
    clips, frames_len = frame_mask.shape
    frames = jnp.arange(frames_len, dtype=jnp.int32)
    valid_grid = (
        (frames[None, :] < lengths[:, None]) & ((frame_mask == 1) | (frames[None, :] == 0))
    ).astype(jnp.float32)
    valid = valid_grid.reshape(-1)
    valid_row = valid[None, :]
    valid_time = jnp.broadcast_to(valid_grid.T[:, :, None], (frames_len, clips, width)).reshape(
        frames_len, clips * width
    )
    count_local = jnp.sum(valid)

    def to_time(array):
        return jnp.transpose(array.reshape(width, clips, frames_len), (2, 1, 0)).reshape(
            frames_len, clips * width
        )

    def from_time(array):
        return jnp.transpose(array.reshape(frames_len, clips, width), (2, 1, 0)).reshape(
            width, slots
        )

    layer_in = inputs
    saved = []
    for layer_no in range(LAYERS):
        weight = weights[layer_no]
        gathered = lax.all_gather(layer_in, "neuron", axis=0, tiled=True)
        pre_norm = add_piece(weight, gathered)
        first_sum, count = lax.psum((jnp.sum(valid_row * pre_norm, axis=1), count_local), "batch")
        mean = first_sum / count
        centered = pre_norm - mean[:, None]
        var = lax.psum(jnp.sum(valid_row * centered * centered, axis=1), "batch") / count
        inv_std = lax.rsqrt(var + EPS)
        zhat = (pre_norm - mean[:, None]) * inv_std[:, None]
        drive = gains[layer_no][:, None] * zhat + (shifts[layer_no] + biases[layer_no])[:, None]
        drive_time = to_time(drive)
        decay_wide = jnp.tile(decays[layer_no], clips)
        start_state = jnp.zeros((clips * width,), jnp.float32)
        _, states = lax.scan(
            partial(recur_step, decay_wide), start_state, (drive_time, valid_time), unroll=8
        )
        saved.append((gathered, zhat, inv_std, drive_time, states, count))
        layer_in = layer_in + valid_row * from_time(states)
    upstream = grad_out
    grad_parts = [None] * LAYERS
    for layer_no in range(LAYERS - 1, -1, -1):
        gathered, zhat, inv_std, drive_time, states, count = saved[layer_no]
        decay_wide = jnp.tile(decays[layer_no], clips)
        gain = gains[layer_no]
        previous = jnp.concatenate([jnp.zeros_like(states[:1]), states[:-1]], axis=0)
        pre_time = drive_time + decay_wide[None, :] * previous
        grad_state = to_time(valid_row * upstream)
        start_carry = jnp.zeros((clips * width,), jnp.float32)
        _, grad_pre_time = lax.scan(
            partial(back_step, decay_wide),
            start_carry,
            (grad_state, valid_time, pre_time),
            reverse=True,
            unroll=8,
        )
        decay_local = jnp.sum(
            jnp.sum(grad_pre_time * previous, axis=0).reshape(clips, width), axis=0
        )
        grad_pre = from_time(grad_pre_time)
        gain_local = jnp.sum(grad_pre * zhat, axis=1)
        shift_local = jnp.sum(grad_pre, axis=1)
        grad_gain, grad_shift, grad_decay = lax.psum(
            (gain_local, shift_local, decay_local), "batch"
        )
        grad_pre_norm = (gain * inv_std)[:, None] * (
            grad_pre - valid_row * (grad_shift[:, None] + zhat * grad_gain[:, None]) / count
        )
        weight_local = weight_columns(grad_pre_norm, gathered)
        input_terms = jnp.einsum("jk,jf->kf", weights[layer_no], grad_pre_norm, precision=HIGH)
        input_grad = lax.psum_scatter(input_terms, "neuron", scatter_dimension=0, tiled=True)
        grad_weight = lax.psum(weight_local, "batch")
        upstream = upstream + input_grad
        grad_parts[layer_no] = (grad_weight, grad_gain, grad_shift, grad_decay)
    grad_weights = jnp.stack([grad_parts[layer_no][0] for layer_no in range(LAYERS)])
    grad_gains = jnp.stack([grad_parts[layer_no][1] for layer_no in range(LAYERS)])
    grad_shifts = jnp.stack([grad_parts[layer_no][2] for layer_no in range(LAYERS)])
    grad_decays = jnp.stack([grad_parts[layer_no][3] for layer_no in range(LAYERS)])
    return (layer_in, upstream, grad_weights, grad_gains, grad_shifts, grad_decays, grad_shifts)


def solution(mesh):
    if (mesh.shape["batch"], mesh.shape["neuron"]) == (4, 8):
        cut = Mesh(mesh.devices.reshape(2, 2, 2, 2, 2), ("y", "x", "h", "l", "c"))
        batch, neuron, body = ("y", "x"), ("h", "l", "c"), half_features
    else:
        cut, batch, neuron, body = mesh, "batch", "neuron", split_features
    in_specs = (
        P(neuron, batch),
        P(None, neuron, None),
        P(None, neuron),
        P(None, neuron),
        P(None, neuron),
        P(None, neuron),
        P(batch),
        P(batch, None),
        P(neuron, batch),
    )
    out_specs = (
        P(neuron, batch),
        P(neuron, batch),
        P(None, neuron, None),
        P(None, neuron),
        P(None, neuron),
        P(None, neuron),
        P(None, neuron),
    )
    return jax.shard_map(
        body, mesh=cut, in_specs=in_specs, out_specs=out_specs, check_vma=False
    )
```

```python
from functools import partial
import math

import jax
import jax.numpy as jnp
from jax import lax
from jax.experimental import pallas as pl
from jax.experimental.pallas import tpu as pltpu
from jax.sharding import Mesh, PartitionSpec as P

LAYERS = 2
EPS = 1e-05
HIGH = lax.Precision.HIGHEST
ROOT_TWO = math.sqrt(2.0)
ROOT_TWO_PI = math.sqrt(2.0 * math.pi)
F32 = jnp.float32
BF16 = jnp.bfloat16
LANES = 128
VMEM_LIMIT = 24 * 1024 * 1024
SMEM_SPEC = pl.BlockSpec(memory_space=pltpu.SMEM)
VMEM_SPEC = pl.BlockSpec(memory_space=pltpu.VMEM)


FLIP2 = [(0, 1), (1, 0)]
DIAGONAL = [(0, 3), (1, 2), (2, 1), (3, 0)]


def swap_half(array):
    return lax.ppermute(array, "l", FLIP2)


def after(value, *others):
    return lax.optimization_barrier((value, others))[0]


def split(value):
    high = value.astype(BF16)
    return high, (value - high.astype(F32)).astype(BF16)


def dot(a, b, dims):
    return lax.dot_general(a, b, (dims, ((), ())), preferred_element_type=F32)


NT = ((1,), (1,))
NN = ((1,), (0,))


def in_hbm(array):
    return pltpu.with_memory_space_constraint(array, pltpu.HBM)


def call(body, out_shape, hbm_outs=(), **kwargs):
    if hbm_outs:
        out_shape = [
            pltpu.HBM(a.shape, a.dtype) if i in hbm_outs else a for i, a in enumerate(out_shape)
        ]
    return pl.pallas_call(
        body,
        out_shape=out_shape,
        compiler_params=pltpu.CompilerParams(vmem_limit_bytes=VMEM_LIMIT),
        **kwargs,
    )


def cost(flops, byte_count):
    return pl.CostEstimate(flops=int(flops) // 64, bytes_accessed=int(byte_count) // 64, transcendentals=0)


def pack_body(frames, place_ref, in_ref, near_ref, far_ref, turned):
    slots = in_ref.shape[1]
    for start in range(0, slots, LANES):
        turned[start : start + LANES, :] = in_ref[:, start : start + LANES].T
    for rel in range(4):
        first = pl.multiple_of(place_ref[rel] * frames, 8)
        out = (near_ref, far_ref)[rel // 2]
        out[(rel % 2) * frames : (rel % 2 + 1) * frames, :] = turned[pl.ds(first, frames), :]


def pack(place, array, frames, waits=False):
    width, slots = array.shape
    out = jax.ShapeDtypeStruct((2 * frames, width), F32)
    return call(
        partial(pack_body, frames),
        grid=(1,),
        out_shape=[out, out],
        in_specs=[SMEM_SPEC, pl.BlockSpec((width, slots), lambda i: (0, 0))],
        out_specs=[pl.BlockSpec(out.shape, lambda i: (0, 0))] * 2,
        scratch_shapes=[pltpu.VMEM((slots, width), F32)],
        hbm_outs=(0, 1) if waits else (),
        cost_estimate=cost(0, 8 * width * slots),
        name="pack",
    )(place, in_hbm(array))


def part_spec(part, frames):
    array, i = part
    if i is None:
        return pl.BlockSpec(array.shape, lambda *_: (0,) * array.ndim)
    return pl.BlockSpec((frames, array.shape[1]), lambda *_: (i, 0))


def arrays_of(parts):
    return [array for array, _ in parts]


def unpack_body(frames, place_ref, *refs):
    ins, out_ref, turned = refs[:4], refs[4], refs[5]
    slots = out_ref.shape[1]
    for rel in range(4):
        first = pl.multiple_of(place_ref[rel] * frames, 8)
        turned[pl.ds(first, frames), :] = ins[rel][...]
    for start in range(0, slots, LANES):
        out_ref[:, start : start + LANES] = turned[start : start + LANES, :].T


def unpack(place, parts, frames, waited=False):
    width = parts[0][0].shape[1]
    slots = 4 * frames
    return call(
        partial(unpack_body, frames),
        grid=(1,),
        out_shape=jax.ShapeDtypeStruct((width, slots), F32),
        in_specs=[SMEM_SPEC] + [part_spec(part, frames) for part in parts],
        out_specs=pl.BlockSpec((width, slots), lambda i: (0, 0)),
        scratch_shapes=[pltpu.VMEM((slots, width), F32)],
        cost_estimate=cost(0, 8 * width * slots),
        name="unpack",
    )(place, *[in_hbm(a) if waited else a for a in arrays_of(parts)])


def merge_body(turn, kept_ref, come_ref, out_ref):
    frames, columns = kept_ref.shape
    width = columns // 2
    for i in range(2):
        some = slice((i ^ turn) * width, ((i ^ turn) + 1) * width)
        out_ref[i * frames : (i + 1) * frames, :] = kept_ref[:, some] + come_ref[:, some]


def merge(kept, half, come, turn=0):
    frames, columns = come.shape
    return call(
        partial(merge_body, turn),
        grid=(1,),
        out_shape=jax.ShapeDtypeStruct((2 * frames, columns // 2), F32),
        in_specs=[
            pl.BlockSpec((frames, columns), lambda i: (0, half)),
            pl.BlockSpec((frames, columns), lambda i: (0, 0)),
        ],
        out_specs=pl.BlockSpec((2 * frames, columns // 2), lambda i: (0, 0)),
        cost_estimate=cost(0, 12 * frames * columns),
        name="merge",
    )(kept, come)


def project_body(n_parts, n_flat, spots, n_weights, first, with_acc, with_stats, with_params, cols_ref, place_ref, *refs):
    del cols_ref

    def take(n):
        nonlocal refs
        some, refs = refs[:n], refs[n:]
        return some

    parts, flat_parts, weights = take(n_parts), take(n_flat), take(n_weights)
    acc, valid, stats_in, params = take(with_acc), take(with_stats > 0), take(with_stats > 1), take(with_params)
    (out_ref,) = take(1)
    stats, flat = take(with_stats > 0), take(n_flat > 0)
    x_high, x_low, far_ref = refs
    step = pl.program_id(0)
    width = x_high.shape[2]

    @pl.when(step == 0)
    def _():
        for block, part in zip(spots, parts):
            for start in range(0, part.shape[1], width):
                high, low = split(part[:, start : start + width])
                x_high[block + start // width] = high
                x_low[block + start // width] = low
        column = 0
        for part in flat_parts:
            flat[0][:, column : column + part.shape[1]] = part[...]
            column += part.shape[1]
        if with_acc:
            out_ref[...] = acc[0][...]
        else:
            out_ref[...] = jnp.zeros_like(out_ref)

    stacked = jnp.concatenate([x_high[step], x_low[step], x_high[step]], axis=1)
    for block, weight in enumerate(weight_blocks(place_ref, weights, far_ref)):
        w_high, w_low = split(weight)
        columns = slice(block * width, (block + 1) * width)
        out_ref[:, columns] += dot(stacked, jnp.concatenate([w_high, w_high, w_low], axis=1), NT)

    if with_stats:
        (stats_ref,) = stats

        @pl.when(step == pl.num_programs(0) - 1)
        def _():
            if stats_in:
                stats_ref[...] = stats_in[0][...]
            own = jnp.sum(valid[0][...], axis=0, keepdims=True)
            per = width // LANES
            for row in range(out_ref.shape[1] // LANES):
                z = out_ref[:, row * LANES : (row + 1) * LANES]
                total = jnp.sum(valid[0][...] * z, axis=0, keepdims=True)
                centred = valid[0][...] * (z - total / own)
                squares = jnp.sum(centred * centred, axis=0, keepdims=True)
                at = place_ref[first + row // per] * per + row % per
                stats_ref[0, pl.ds(at, 1), :] = total
                stats_ref[1, pl.ds(at, 1), :] = squares
                stats_ref[2, pl.ds(at, 1), :] = own
            if with_params:
                rest = params[0].shape[0] - 8
                stats_ref[3] = params[0][:8, :]
                stats_ref[4] = jnp.zeros_like(stats_ref[4])
                stats_ref[4, :rest, :] = params[0][8:, :]


def weight_specs(weights, layer, pairs=2):
    specs = []
    for weight in weights:
        if weight.ndim == 3:
            shape = (1, weight.shape[1], pairs * weight.shape[1])
            specs.append(pl.BlockSpec(shape, lambda s, cols, *_: (layer, 0, cols[s])))
        else:
            shape = (weight.shape[0], pairs * 4 * weight.shape[0])
            specs.append(pl.BlockSpec(shape, lambda s, cols, *_: (0, cols[s])))
    return specs


def far_scratch(width, pairs=2):
    return pltpu.VMEM((2, width, pairs * width), F32)


def weight_blocks(place_ref, refs, far_ref):
    near = [ref[0] for ref in refs if len(ref.shape) == 3]
    pieces = [ref for ref in refs if len(ref.shape) == 2]
    far = []
    for i in range(len(pieces) // 4):
        for rel, piece in enumerate(pieces[4 * i : 4 * i + 4]):
            rows = piece.shape[0]
            row = 2 * (place_ref[4] ^ (rel // 2)) + (place_ref[5] ^ (rel % 2))
            far_ref[i, pl.ds(pl.multiple_of(row * rows, rows), rows), :] = piece[...]
        far.append(far_ref[i])
    return near + far


def project(
    place, frames, parts, blocks, weights, layer, acc=None, valid=None, stats=None, params=None, flat=()
):
    near = weights[0].ndim == 3
    units = sum(1 if w.ndim == 3 else 0.25 for w in weights)
    width = weights[0].shape[1] if near else 4 * weights[0].shape[0]
    n = blocks.shape[0]
    spots, block = [], 0
    for array, _ in parts:
        spots.append(block)
        block += array.shape[1] // width
    full = pl.BlockSpec(memory_space=pltpu.VMEM)
    in_specs = [part_spec(part, frames) for part in (*parts, *flat)]
    in_specs += weight_specs(weights, layer, 1)
    operands = arrays_of(parts) + arrays_of(flat) + [in_hbm(w) for w in weights]
    array = jax.ShapeDtypeStruct((frames, int(units) * width), F32)
    array_spec = pl.BlockSpec(array.shape, lambda s, cols, place: (0, 0))
    out_shape, out_specs = [array], [array_spec]
    if acc is not None:
        in_specs.append(array_spec)
        operands.append(in_hbm(acc))
    if valid is not None:
        in_specs.append(full)
        operands.append(valid)
        shape = (3 if params is None else 5, 4 * width // LANES, LANES)
        out_shape.append(jax.ShapeDtypeStruct(shape, F32))
        out_specs.append(pl.BlockSpec(shape, lambda s, cols, place: (0, 0, 0)))
    for extra in (stats, params):
        if extra is not None:
            in_specs.append(full)
            operands.append(extra)
    if flat:
        out_shape.append(jax.ShapeDtypeStruct((frames, 4 * width), F32))
        out_specs.append(pl.BlockSpec((frames, 4 * width), lambda s, cols, place: (0, 0)))
    return call(
        partial(
            project_body,
            len(parts),
            len(flat),
            spots,
            len(weights),
            0 if near else 2,
            acc is not None,
            (valid is not None) + (stats is not None),
            params is not None,
        ),
        grid_spec=pltpu.PrefetchScalarGridSpec(
            num_scalar_prefetch=2,
            grid=(n,),
            in_specs=in_specs,
            out_specs=out_specs,
            scratch_shapes=[pltpu.VMEM((n, frames, width), BF16)] * 2 + [far_scratch(width, 1)],
        ),
        out_shape=out_shape,
        hbm_outs=(0, len(out_shape) - 1) if flat else (0,),
        cost_estimate=cost(6 * frames * n * width * units * width, 4 * n * width * units * width),
        name="project",
    )(blocks, place, *operands)


def to_relative(place_ref, spread, rows_ref, value, slot):
    per = value.shape[0] // 4
    spread[...] = value
    for rel in range(4):
        first = place_ref[rel] * per
        for row in range(per):
            rows_ref[slot, rel * per + row : rel * per + row + 1, :] = spread[
                pl.ds(first + row, 1), :
            ]


def tree(values):
    while len(values) > 1:
        values = [a + b for a, b in zip(values[::2], values[1::2])]
    return values[0]


def gathered(ref, slot):
    return [ref[i] for i in range(slot, ref.shape[0], ref.shape[0] // 16)]


def norm_terms(stats_ref):
    each = [gathered(stats_ref, slot) for slot in range(3)]
    totals, squares, owns = each
    count = tree(owns)
    mean = tree(totals) / count
    away = [total / own - mean for total, own in zip(totals, owns)]
    spread = tree([s + n * a * a for s, n, a in zip(squares, owns, away)])
    return count, mean, lax.rsqrt(spread / count + EPS)


CHUNKS = 4


def columns_of(refs, row):
    for ref in refs:
        if row * LANES < ref.shape[1]:
            return ref[:, row * LANES : (row + 1) * LANES]
        row -= ref.shape[1] // LANES


def recur_body(n_z, last, layer, spread_params, place_ref, gate_ref, *refs):
    z_refs, refs = refs[:n_z], refs[n_z:]
    (stats_ref, params_ref, valid_ref, x_ref), refs = refs[:4], refs[4:]
    outs, refs = refs[: 1 + 3 * last], refs[1 + 3 * last :]
    if spread_params:
        state_ref, slope_ref, params_out, rows, spread, held, drive_s, state_s, slope_s = refs
    else:
        state_ref, slope_ref, rows, spread, held, drive_s, state_s, slope_s = refs
    frames, features = x_ref.shape
    blocks = features // LANES
    per = blocks // 4
    chunk = pl.program_id(0)

    @pl.when(chunk == 0)
    def _():
        if spread_params:
            for rel in range(4):
                first = place_ref[rel] * (stats_ref.shape[0] // 16) + 3
                for row in range(LAYERS * 3 * per):
                    at = rel * per + row % per
                    params_out[row // per, at : at + 1, :] = stats_ref[
                        first + row // 8, row % 8 : row % 8 + 1, :
                    ]
            params = [params_out[3 * layer + i] for i in range(3)]
        else:
            params = [params_ref[3 * layer + i] for i in range(3)]
        _, mean, inv_std = norm_terms(stats_ref)
        to_relative(place_ref, spread, rows, mean, 0)
        to_relative(place_ref, spread, rows, inv_std, 1)
        rows[1] = rows[1] * params[0]
        rows[2] = params[1]
        rows[3] = params[2]
        held[...] = jnp.zeros_like(held)

    for row in range(blocks):
        drive_s[row * frames : (row + 1) * frames, :] = (
            columns_of(z_refs, row) - rows[0, row : row + 1, :]
        ) * rows[1, row : row + 1, :] + rows[2, row : row + 1, :]
    decay = rows[3]

    def step(t, state):
        at = pl.ds(t, blocks, stride=frames)
        pre = drive_s[at, :] + decay * state
        half = 0.5 + 0.5 * lax.erf(pre * (1.0 / ROOT_TWO))
        gate = gate_ref[chunk * frames + t] > 0.0
        slope = half + pre * jnp.exp(-0.5 * pre * pre) * (1.0 / ROOT_TWO_PI)
        state = jnp.where(gate, pre * half, state)
        state_s[at, :] = state
        slope_s[at, :] = jnp.where(gate, slope, 0.0)
        return state

    held[...] = lax.fori_loop(0, frames, step, held[...], unroll=8)
    valid = valid_ref[...]
    for row in range(blocks):
        lanes = slice(row * LANES, (row + 1) * LANES)
        state = state_s[row * frames : (row + 1) * frames, :]
        state_ref[:, lanes] = state
        slope_ref[:, lanes] = slope_s[row * frames : (row + 1) * frames, :]
        value = x_ref[:, lanes] + valid * state
        out, at = (outs[row // per], row % per) if last else (outs[0], row)
        out[:, at * LANES : (at + 1) * LANES] = value


def recur(layer, place, gate, z, stats, params, valid, x, last):
    frames, features = x.shape
    blocks = features // LANES
    some = frames // CHUNKS
    whole = lambda array: pl.BlockSpec(array.shape, lambda i: (0,) * array.ndim)
    by_chunk = lambda array: pl.BlockSpec((some, array.shape[1]), lambda i: (i, 0))
    full = jax.ShapeDtypeStruct((frames, features), F32)
    piece = jax.ShapeDtypeStruct((frames, features // 4), F32)
    out_shape = [piece] * 4 if last else [full]
    out_shape += [full, full]
    out_specs = [by_chunk(a) for a in out_shape]
    spread_params = params is None
    if spread_params:
        out_shape.append(jax.ShapeDtypeStruct((3 * LAYERS, blocks, LANES), F32))
        out_specs.append(whole(out_shape[-1]))
        params = valid
    return call(
        partial(recur_body, len(z), last, layer, spread_params),
        grid=(CHUNKS,),
        in_specs=[SMEM_SPEC, SMEM_SPEC]
        + [by_chunk(a) for a in z]
        + [whole(a) for a in (stats, params)]
        + [by_chunk(a) for a in (valid, x)],
        out_specs=out_specs,
        out_shape=out_shape,
        hbm_outs=tuple(range(len(out_shape) - spread_params)) if last else (1, 2),
        scratch_shapes=[
            pltpu.VMEM((4, blocks, LANES), F32),
            pltpu.VMEM((blocks, LANES), F32),
            pltpu.VMEM((blocks, LANES), F32),
        ]
        + [pltpu.VMEM((blocks * some, LANES), F32)] * 3,
        cost_estimate=cost(100 * frames * features, 20 * frames * features),
        name="recur",
    )(place, gate, *[in_hbm(a) for a in z], stats, params, valid, in_hbm(x))


def back_body(n_z, n_ups, spots, layer, place_ref, gate_ref, *refs):
    z_refs, refs = refs[:n_z], refs[n_z:]
    (stats_ref, params_ref), refs = refs[:2], refs[2:]
    ups, (state_ref, slope_ref), refs = refs[:n_ups], refs[n_ups : n_ups + 2], refs[n_ups + 2 :]
    grad_ref, sums_ref, rows, spread, held, up_s, state_s, slope_s = refs
    frames, features = state_ref.shape
    blocks = features // LANES
    per = blocks // 4
    tall = frames + 8
    step_no = pl.program_id(0)
    chunk = pl.num_programs(0) - 1 - step_no

    @pl.when(step_no == 0)
    def _():
        _, mean, inv_std = norm_terms(stats_ref)
        to_relative(place_ref, spread, rows, mean, 0)
        to_relative(place_ref, spread, rows, inv_std, 1)
        held[...] = jnp.zeros_like(held)

    for row in range(blocks):
        lanes = slice(row * LANES, (row + 1) * LANES)
        base = row * frames
        up = None
        for (_, column), part in zip(spots, ups):
            if column <= row * LANES < column + part.shape[1]:
                value = part[:, row * LANES - column : (row + 1) * LANES - column]
                up = value if up is None else up + value
        up_s[base : base + frames, :] = up
        state_s[row * tall : row * tall + 8, :] = jnp.zeros((8, LANES), F32)
        state_s[row * tall + 8 : (row + 1) * tall, :] = state_ref[:, lanes]
        slope_s[base : base + frames, :] = slope_ref[:, lanes]
    decay = params_ref[3 * layer + 2]

    def step(i, carry):
        t = frames - 1 - i
        at = pl.ds(t, blocks, stride=frames)
        slope = slope_s[at, :]
        gate = gate_ref[chunk * frames + t]
        total = gate * up_s[at, :] + carry
        up_s[at, :] = total * slope
        return total * (slope * decay + (1.0 - gate))

    held[0] = lax.fori_loop(0, frames, step, held[0], unroll=8)
    held[4] += held[1] * state_s[pl.ds(tall - 1, blocks, stride=tall), :]
    held[1] = up_s[pl.ds(0, blocks, stride=frames), :]
    for row in range(blocks):
        lanes = slice(row * LANES, (row + 1) * LANES)
        grad = up_s[row * frames : (row + 1) * frames, :]
        grad_ref[:, lanes] = grad
        zhat = (columns_of(z_refs, row) - rows[0, row : row + 1, :]) * rows[1, row : row + 1, :]
        before = state_s[row * tall + 7 : row * tall + 7 + frames, :]
        for slot, value in enumerate((grad * zhat, grad, grad * before)):
            held[2 + slot, row : row + 1, :] += jnp.sum(value, axis=0, keepdims=True)

    @pl.when(chunk == 0)
    def _():
        for row in range(blocks):
            at = place_ref[row // per] * per + row % per
            for slot in range(3):
                sums_ref[slot, pl.ds(at, 1), :] = held[2 + slot, row : row + 1, :]


def spots_of_sum(parts, width):
    spots, column = [], 0
    for array, _ in parts:
        spots.append((0, column % (4 * width)))
        column += array.shape[1]
    return spots


def back(layer, place, gate, z, stats, params, ups, states, slopes):
    frames, features = states.shape
    width = features // 4
    blocks = features // LANES
    some = frames // CHUNKS
    whole = lambda array: pl.BlockSpec(array.shape, lambda i: (0,) * array.ndim)

    def by_chunk(array, first=0):
        return pl.BlockSpec(
            (some, array.shape[1]), lambda i: ((first or 0) * CHUNKS + CHUNKS - 1 - i, 0)
        )

    out_shape = [
        jax.ShapeDtypeStruct((frames, features), F32),
        jax.ShapeDtypeStruct((3, blocks, LANES), F32),
    ]
    return call(
        partial(back_body, len(z), len(ups), spots_of_sum(ups, width), layer),
        grid=(CHUNKS,),
        in_specs=[SMEM_SPEC] * 2
        + [by_chunk(a) for a in z]
        + [whole(a) for a in (stats, params)]
        + [by_chunk(*up) for up in ups]
        + [by_chunk(a) for a in (states, slopes)],
        out_specs=[by_chunk(out_shape[0]), whole(out_shape[1])],
        out_shape=out_shape,
        scratch_shapes=[
            pltpu.VMEM((2, blocks, LANES), F32),
            pltpu.VMEM((blocks, LANES), F32),
            pltpu.VMEM((5, blocks, LANES), F32),
            pltpu.VMEM((blocks * some, LANES), F32),
            pltpu.VMEM((blocks * (some + 8), LANES), F32),
            pltpu.VMEM((blocks * some, LANES), F32),
        ],
        cost_estimate=cost(30 * frames * features, 20 * frames * features),
        name="back",
    )(
        place,
        gate,
        *[in_hbm(a) for a in z],
        stats,
        params,
        *arrays_of(ups),
        in_hbm(states),
        in_hbm(slopes),
    )


def input_terms(high_s, low_s, weights):
    left, right = [], []
    for block, weight in enumerate(weights):
        w_high, w_low = split(weight)
        left += [high_s[block], low_s[block], high_s[block]]
        right += [w_high, w_high, w_low]
    return dot(jnp.concatenate(left, axis=1), jnp.concatenate(right, axis=0), NN)


def norm_back_body(n_z, split_terms, layer, cols_ref, place_ref, grad_ref, *refs):
    del cols_ref
    z_refs, refs = refs[:n_z], refs[n_z:]
    params_ref, valid_ref, stats_ref, sums_ref, *refs = refs
    weights, refs = refs[:10], refs[10:]
    if split_terms:
        out_ref, leave_ref, near_term_ref, far_term_ref, sums_out_ref, *refs = refs
        term_refs, starts = (far_term_ref, near_term_ref), (0, 0)
    else:
        out_ref, leave_ref, term_ref, sums_out_ref, *refs = refs
        term_refs, starts = (term_ref, term_ref), (2 * grad_ref.shape[1] // 4, 0)
    rows, spread, high_s, low_s, far_ref = refs
    blocks = grad_ref.shape[1] // LANES
    width = high_s.shape[2]
    per = width // LANES

    @pl.when(pl.program_id(0) == 0)
    def _():
        count, mean, inv_std = norm_terms(stats_ref)
        to_relative(place_ref, spread, rows, mean, 0)
        to_relative(place_ref, spread, rows, inv_std, 1)
        rows[2] = rows[1] * params_ref[3 * layer]
        sums = [tree(gathered(sums_ref, slot)) for slot in range(3)]
        for slot in range(3):
            sums_out_ref[slot] = sums[slot]
        to_relative(place_ref, spread, rows, sums[0] / count, 3)
        to_relative(place_ref, spread, rows, sums[1] / count, 4)
        valid = valid_ref[...]
        for row in range(blocks):
            lanes = slice(row * LANES, (row + 1) * LANES)
            one = lambda slot: rows[slot, row : row + 1, :]
            zhat = (columns_of(z_refs, row) - one(0)) * one(1)
            value = one(2) * (grad_ref[:, lanes] - valid * (one(4) + zhat * one(3)))
            out_ref[:, lanes] = value
            if (row // per) % 2:
                at = (row // per // 2) * width + (row % per) * LANES
                leave_ref[:, at : at + LANES] = value
            high, low = split(value)
            inner = slice((row % per) * LANES, (row % per + 1) * LANES)
            high_s[row // per, :, inner] = high
            low_s[row // per, :, inner] = low

    value = input_terms(high_s, low_s, weight_blocks(place_ref, weights, far_ref))
    for step, (term_ref, first) in enumerate(zip(term_refs, starts)):

        @pl.when(pl.program_id(0) == step)
        def _():
            for pair in range(2):
                at = pl.multiple_of(((place_ref[0] & 1) ^ pair) * width, width)
                term_ref[:, pl.ds(first + at, width)] = value[
                    :, pair * width : (pair + 1) * width
                ]


def norm_back(columns, place, grad, z, params, valid, stats, sums, weights, layer, split_terms):
    frames, features = grad.shape
    width = features // 4
    blocks = features // LANES
    whole = lambda array: pl.BlockSpec(array.shape, lambda s, cols, place: (0,) * array.ndim)
    operands = [grad, *[in_hbm(a) for a in z], params, valid, stats, sums]
    full = jax.ShapeDtypeStruct((frames, features), F32)
    half = jax.ShapeDtypeStruct((frames, 2 * width), F32)
    terms = [half, half] if split_terms else [full]
    out_shape = [full, half, *terms, jax.ShapeDtypeStruct((3, blocks, LANES), F32)]
    return call(
        partial(norm_back_body, len(z), split_terms, layer),
        grid_spec=pltpu.PrefetchScalarGridSpec(
            num_scalar_prefetch=2,
            grid=(2,),
            in_specs=[whole(a) for a in operands] + weight_specs(weights, layer),
            out_specs=[whole(a) for a in out_shape],
            scratch_shapes=[
                pltpu.VMEM((5, blocks, LANES), F32),
                pltpu.VMEM((blocks, LANES), F32),
                pltpu.VMEM((4, frames, width), BF16),
                pltpu.VMEM((4, frames, width), BF16),
                far_scratch(width),
            ],
        ),
        out_shape=out_shape,
        hbm_outs=(0,),
        cost_estimate=cost(6 * frames * features * features, 4 * features * features),
        name="norm_back",
    )(columns, place, *operands, *[in_hbm(w) for w in weights])


def own_terms_body(n_ups, spots, cols_ref, place_ref, grad_ref, *refs):
    del cols_ref
    ups, refs = refs[:n_ups], refs[n_ups:]
    weights, refs = refs[:10], refs[10:]
    out_ref, high_s, low_s, far_ref = refs
    width = high_s.shape[2]
    step = pl.program_id(0)

    @pl.when(step == 0)
    def _():
        for block in range(4):
            high, low = split(grad_ref[:, block * width : (block + 1) * width])
            high_s[block] = high
            low_s[block] = low

    value = input_terms(high_s, low_s, weight_blocks(place_ref, weights, far_ref))
    for pair in range(2):
        at = pl.multiple_of(((place_ref[0] & 1) ^ pair) * width, width)
        out_ref[:, pl.ds(at, width)] = value[:, pair * width : (pair + 1) * width]
    for half in range(2):

        @pl.when(step == half)
        def _():
            first = 2 * half * width
            for (_, column), up in zip(spots, ups):
                low = max(column, first)
                high = min(column + up.shape[1], first + 2 * width)
                if low < high:
                    out_ref[:, low - first : high - first] += up[:, low - column : high - column]


def own_terms(columns, place, grad, ups, weights, layer):
    frames, features = grad.shape
    width = features // 4
    whole = lambda array: pl.BlockSpec(array.shape, lambda s, cols, place: (0,) * array.ndim)
    step_block = pl.BlockSpec((frames, 2 * width), lambda s, cols, place: (0, s))
    return call(
        partial(own_terms_body, len(ups), spots_of_sum(ups, width)),
        grid_spec=pltpu.PrefetchScalarGridSpec(
            num_scalar_prefetch=2,
            grid=(2,),
            in_specs=[whole(grad)]
            + [part_spec(up, frames) for up in ups]
            + weight_specs(weights, layer),
            out_specs=step_block,
            scratch_shapes=[pltpu.VMEM((4, frames, width), BF16)] * 2 + [far_scratch(width)],
        ),
        out_shape=jax.ShapeDtypeStruct((frames, features), F32),
        cost_estimate=cost(6 * frames * features * features, 4 * features * features),
        name="own_terms",
    )(columns, place, in_hbm(grad), *arrays_of(ups), *[in_hbm(w) for w in weights])


def prepare_body(lists_ref, place_ref, own_ref, near_ref, high_ref, low_ref):
    del lists_ref
    padded = high_ref.shape[0] // 2
    width = high_ref.shape[1] // 2
    for clip, part in enumerate((own_ref, near_ref)):
        rows = part.shape[0]
        for dc in range(2):
            at = pl.multiple_of((place_ref[6] ^ clip ^ dc) * width, width)
            high, low = split(part[:, dc * width : (dc + 1) * width])
            high_ref[clip * padded : clip * padded + rows, pl.ds(at, width)] = high
            low_ref[clip * padded : clip * padded + rows, pl.ds(at, width)] = low
        zeros = jnp.zeros((padded - rows, 2 * width), BF16)
        high_ref[clip * padded + rows : (clip + 1) * padded, :] = zeros
        low_ref[clip * padded + rows : (clip + 1) * padded, :] = zeros


def prepare(place, own, near):
    frames, features = own.shape
    width = features // 4
    padded = -(-frames // LANES) * LANES
    in_spec = pl.BlockSpec((frames, 2 * width), lambda s, *_: (0, s))
    out = jax.ShapeDtypeStruct((2 * padded, features), BF16)
    out_spec = pl.BlockSpec((2 * padded, 2 * width), lambda s, order, place: (0, order[s]))
    order = jnp.stack([place[0] >> 1, 1 - (place[0] >> 1)])
    return call(
        prepare_body,
        grid_spec=pltpu.PrefetchScalarGridSpec(
            num_scalar_prefetch=2,
            grid=(2,),
            in_specs=[in_spec, in_spec],
            out_specs=[out_spec, out_spec],
        ),
        out_shape=[out, out],
        hbm_outs=(0, 1),
        cost_estimate=cost(0, 16 * frames * features),
        name="prepare",
    )(order, place, in_hbm(own), in_hbm(near))


def product(g_high, g_low, x_high, x_low):
    return dot(g_high, x_high, NN) + (dot(g_high, x_low, NN) + dot(g_low, x_high, NN))


def weight_body(turn, place_ref, *refs):
    if turn:
        grad_ref, near_ref, x_high, x_low, kept, sent, g_high, g_low, t_high, t_low = refs

        @pl.when(pl.program_id(0) == 0)
        def _():
            frames, features = grad_ref.shape
            width = features // 4
            rows = width // 4
            padded = t_high.shape[1] // 2
            t_high[...] = jnp.zeros_like(t_high)
            t_low[...] = jnp.zeros_like(t_low)
            for clip in range(2):
                for dh in range(2):
                    if clip == 0:
                        part = grad_ref[:, 2 * dh * width : (2 * dh + 1) * width]
                    else:
                        part = near_ref[:, dh * width : (dh + 1) * width]
                    high, low = split(part.T)
                    at = (
                        slice(dh * width, (dh + 1) * width),
                        slice(clip * padded, clip * padded + frames),
                    )
                    t_high[at] = high
                    t_low[at] = low
            for group in range(8):
                first, second, dh = group // 4, group // 2 % 2, group % 2
                core = place_ref[6]
                y = place_ref[4] ^ (first * core + second * (1 - core))
                x = place_ref[5] ^ (first * (1 - core) + second * core)
                at = pl.multiple_of(dh * width + (2 * y + x) * rows, rows)
                g_high[group * rows : (group + 1) * rows, :] = t_high[pl.ds(at, rows), :]
                g_low[group * rows : (group + 1) * rows, :] = t_low[pl.ds(at, rows), :]

    else:
        g_high, g_low, x_high, x_low, kept, sent = refs
    half = g_high.shape[0] // 2
    value = product(g_high[...], g_low[...], x_high[...], x_low[...])
    kept[...] = value[:half].reshape(kept.shape)
    sent[...] = value[half:].reshape(sent.shape)


def weight_rows(side, place, grads, x_split, width):
    turn = side == 0
    whole = lambda array: pl.BlockSpec(array.shape, lambda s, place: (0,) * array.ndim)
    x_spec = pl.BlockSpec((x_split[0].shape[0], width), lambda s, place: (0, s))
    shape = (2, 2, width // 4, 4 * width)
    out_shape = [jax.ShapeDtypeStruct(shape, F32)] * 2
    out_specs = [pl.BlockSpec(shape[:3] + (width,), lambda s, place: (0, 0, 0, s))] * 2
    scratch = []
    if turn:
        turned = (2 * width, x_split[0].shape[0])
        out_shape += [jax.ShapeDtypeStruct(turned, BF16)] * 2
        out_specs += [whole(out_shape[-1])] * 2
        scratch = [pltpu.VMEM(turned, BF16)] * 2
    return call(
        partial(weight_body, turn),
        grid_spec=pltpu.PrefetchScalarGridSpec(
            num_scalar_prefetch=1,
            grid=(4,),
            in_specs=[whole(a) for a in grads] + [x_spec] * 2,
            out_specs=out_specs,
            scratch_shapes=scratch,
        ),
        out_shape=out_shape,
        hbm_outs=(0,),
        cost_estimate=cost(12 * x_split[0].shape[0] * width * 4 * width, 4 * 8 * width * width),
        name="weight_rows",
    )(place, *([in_hbm(grads[0]), grads[1]] if turn else grads), *[in_hbm(x) for x in x_split])


def step_body(n, widths, cut, *refs):
    ins, outs = refs[: 2 * n], refs[2 * n :]
    starts = [sum(widths[:i]) for i in range(len(widths))]
    column = 0
    for i in range(n):
        total = ins[2 * i][...] + ins[2 * i + 1][...]
        end = column + total.shape[-1]
        for j, (start, columns) in enumerate(zip(starts, widths)):
            low, high = max(start, column), min(start + columns, end)
            if low < high:
                to = (Ellipsis, slice(low - start, high - start))
                piece = total[..., low - column : high - column]
                pieces = [piece]
                for _ in range(cut):
                    pieces = [half[k] for half in pieces for k in range(2)]
                for k, some in enumerate(pieces):
                    outs[len(pieces) * j + k][to] = some
        column = end


def step_of(*pairs, cut=1, widths=None):
    shape = list(pairs[0][0].shape)
    widths = widths or [sum(pair[0].shape[-1] for pair in pairs)]
    outs = []
    for columns in widths:
        shape[-1] = columns
        outs += [jax.ShapeDtypeStruct(tuple(shape[cut:]), F32)] * 2**cut
    whole = lambda array: pl.BlockSpec(array.shape, lambda i: (0,) * array.ndim)
    operands = [array for pair in pairs for array in pair]
    return call(
        partial(step_body, len(pairs), widths, cut),
        grid=(1,),
        in_specs=[whole(a) for a in operands],
        out_specs=[whole(a) for a in outs],
        out_shape=outs,
        cost_estimate=cost(0, 4 * sum(a.size for a in operands)),
        name="reduction_step",
    )(*operands)


def plane_swap(array, step):
    pairs = []
    for i in range(8):
        over_x = (i % 2 == 0) == (step == 0)
        pairs.append((i, i ^ 2 if over_x else i ^ 4))
    return lax.ppermute(array, ("y", "x", "c"), pairs)


def plane_gather(share, *before):
    first = plane_swap(share, 0)
    second = plane_swap(share, 1)
    return [share, second, first, plane_swap(after(first, second, *before), 1)]


def assemble_body(by_core, place_ref, *refs):
    out_ref = refs[-1]
    core = place_ref[6] if by_core else 1
    rows, columns = refs[0].shape
    quarter = columns // 4
    for i in range(4):
        first, second = i // 2, i % 2
        y = place_ref[4] ^ (first * core + second * (1 - core))
        x = place_ref[5] ^ (first * (1 - core) + second * core)
        at = pl.multiple_of((2 * y + x) * rows, rows)
        for side in range(2):
            for h in range(2):
                to = pl.multiple_of((2 * h + (place_ref[7] ^ side)) * quarter, quarter)
                some = slice((2 * side + h) * quarter, (2 * side + h + 1) * quarter)
                out_ref[0, pl.ds(at, rows), pl.ds(to, quarter)] = refs[i][:, some]


def assemble(place, pieces, layer, onto=None, by_core=True):
    rows, columns = 4 * pieces[0].shape[0], pieces[0].shape[1]
    aliases, extra, extra_specs = {}, [], []
    if onto is not None:
        aliases, extra = {1 + len(pieces): 0}, [onto]
        extra_specs = [pl.BlockSpec(memory_space=pl.ANY)]
    (out,) = call(
        partial(assemble_body, by_core),
        grid=(1,),
        out_shape=[jax.ShapeDtypeStruct((LAYERS, rows, columns), F32)],
        hbm_outs=(0,),
        in_specs=[SMEM_SPEC]
        + [pl.BlockSpec(p.shape, lambda i: (0, 0)) for p in pieces]
        + extra_specs,
        out_specs=[pl.BlockSpec((1, rows, columns), lambda i: (layer, 0, 0))],
        input_output_aliases=aliases,
        cost_estimate=cost(0, 8 * rows * columns),
        name="assemble",
    )(place, *[p if extra else in_hbm(p) for p in pieces], *extra)
    return out


def half_features(inputs, weights, gains, shifts, decays, biases, lengths, frame_mask, grad_out):
    width, slots = inputs.shape
    clips, frames = frame_mask.shape
    depth = weights.shape[2]
    blocks = 4 * width // LANES
    y, x, h, l, c = (lax.axis_index(name) for name in ("y", "x", "h", "l", "c"))
    b = 2 * y + x
    numbers = [2 * (h ^ (rel // 2)) + (c ^ (rel % 2)) for rel in range(4)] + [y, x, c, l]
    place = jnp.stack(numbers).astype(jnp.int32)
    own_blocks, other_blocks = (
        jnp.stack(
            [2 * (2 * (h ^ (rel // 2)) + half) + (c ^ (rel % 2)) for rel in range(4)]
        ).astype(jnp.int32)
        for half in (l, 1 - l)
    )
    own_columns = jnp.stack([2 * h + l, 2 * (1 - h) + l]).astype(jnp.int32)
    other_columns = jnp.stack([2 * (1 - h) + 1 - l, 2 * h + 1 - l]).astype(jnp.int32)
    rows = width // 4

    clip = 2 * h + c
    seen = lax.dynamic_index_in_dim(frame_mask, clip, 0, keepdims=False)
    length = lax.dynamic_index_in_dim(lengths, clip, 0, keepdims=False)
    moments = jnp.arange(frames, dtype=jnp.int32)
    gate = ((moments < length) & ((seen == 1) | (moments == 0))).astype(F32)
    valid = jnp.broadcast_to(gate[:, None], (frames, LANES))

    def far_share(layer):
        return lax.dynamic_slice(weights, (layer, b * rows, 0), (1, rows, depth))[0]

    def over_h(array):
        return lax.ppermute(array, "h", FLIP2)

    def over_c(array):
        return lax.ppermute(array, "c", FLIP2)

    def over_second(array):
        return plane_swap(array, 1)

    def four_of(near_rows, far_rows):
        return [
            (near_rows, 0),
            (over_c(near_rows), 1),
            (far_rows, 0),
            (over_c(far_rows), 1),
        ]

    def four_of_plane(share):
        both = lax.ppermute(share, ("y", "x"), DIAGONAL)
        return [share, lax.ppermute(share, "x", FLIP2), lax.ppermute(share, "y", FLIP2), both]

    near = over_c(weights)
    share = far_share(0)
    close, away = pack(place, after(inputs, share), frames)
    share = over_h(share)
    away = over_h(away)
    other_close = swap_half(close)
    up_close, up_away = pack(place, after(grad_out, close), frames, waits=True)
    share = after(share, up_close, valid, near, other_close)
    pieces = four_of_plane(share)
    away = after(away, pieces[1:])
    half_weights = [[weights, near, *pieces, *map(over_c, after(pieces, away))]]
    own = four_of(after(close, away), away)
    other_away = swap_half(away)
    others = [(other_close, 0), (over_c(other_close), 1)]
    params = jnp.stack([gains, shifts + biases, decays], axis=1)
    own_params = params.reshape(LAYERS * 3 * width // LANES, LANES)
    params = None

    def gather(array, axes):
        return lax.all_gather(array, axes, tiled=True)

    weight = half_weights[0]
    early = jnp.concatenate([own_blocks, other_blocks[:2]])
    z, own_flat = project(place, frames, own + others, early, weight, 0, flat=own)
    others += [(other_away, 0), (over_c(after(other_away, z)), 1)]
    z, stats, other_flat = project(
        place,
        frames,
        others[2:],
        other_blocks[2:],
        weight,
        0,
        z,
        valid,
        params=own_params,
        flat=others,
    )
    z = [z]
    stats = gather(stats, ("h", "c"))
    share = over_c(lax.ppermute(after(far_share(1), stats), ("h", "c"), DIAGONAL))
    stats = gather(stats, ("y", "x"))
    x, states, slopes, params = recur(0, place, gate, z, stats, None, valid, own_flat, False)
    own_near, other_near = over_c(after(own_flat, z[0])), over_c(after(other_flat, z[0]))
    x_near = over_c(x)
    own_split = prepare(place, after(own_flat, x_near), own_near)
    other_split = prepare(place, after(other_flat, x_near), other_near)
    saved = [(own_split, other_split, z, stats, states, slopes)]

    pieces = four_of_plane(after(share, slopes, own_near, other_near))
    near = [weights, near]
    other = swap_half(x)
    x_own = after(x, own_split[0], other_split[0])
    z, *_ = project(place, frames, [(x_own, None)], own_blocks, near, 1)
    own_split = prepare(place, after(x, z), x_near)
    far = [*pieces, *map(over_c, after(pieces, own_split[0]))]
    up_away = over_h(after(up_away, other, own_split[0]))
    half_weights.append(near + far)
    z, stats = project(place, frames, [(other, None)], other_blocks, near, 1, z, valid)
    both = jnp.concatenate([own_blocks, other_blocks])
    z_far, stats = project(
        place,
        frames,
        [(x, None), (other, None)],
        both,
        far,
        1,
        None,
        valid,
        stats,
    )
    z = [z, z_far]
    stats = gather(gather(stats, ("y", "x")), ("h", "c"))
    upstream = four_of(up_close, after(up_away, stats))
    *output, states, slopes = recur(1, place, gate, z, stats, params, valid, x, True)
    other_near = over_c(after(other, slopes))
    saved.append((own_split, (other, other_near), z, stats, states, slopes))
    diagonal = over_c(over_h(output[3]))

    ups = upstream
    results = [None] * LAYERS
    for layer in range(LAYERS - 1, -1, -1):
        own_split, other_split, z, stats, states, slopes = saved[layer]
        weight = half_weights[layer]
        grad_pre, sums = back(layer, place, gate, z, stats, params, ups, states, slopes)
        sums = gather(sums, ("y", "x"))
        if layer == 0:
            come[0] = after(come[0], sums, away, output[1][0])
            later, go = step_of((in_hbm(stay[0]), come[0]), (in_hbm(stay[1]), come[1]))
            sums = after(sums, later)
            go = over_second(go)
        sums = gather(sums, ("h", "c"))
        grad_z, leaving, *terms, sums = norm_back(
            other_columns, place, grad_pre, z, params, valid, stats, sums, weight, layer,
            layer == 0,
        )
        leaving = over_c(leaving)
        if layer > 0:
            received = [swap_half(terms[0])]
            other_split = prepare(place, *after(other_split, grad_z))
            leaving = after(leaving, diagonal, other_split[0])
        else:
            received = [None, swap_half(terms[1])]
            later, go = step_of((later, after(go, grad_z)))
            leaving = after(leaving, later)
            go = lax.ppermute(go, ("h", "c"), DIAGONAL)
            later = (later, go)
        *first, g_high, g_low = weight_rows(0, place, (grad_z, leaving), own_split, width)
        turned = (g_high, g_low)
        come = [plane_swap(first[1], 0)]
        if layer == 0:
            received[0] = swap_half(after(terms[0], received[1]))
        second = weight_rows(1, place, turned, other_split, width)
        come.append(plane_swap(second[1], 0))
        stay = (first[0], second[0])
        kept = own_terms(own_columns, place, after(grad_z, second[0]), ups, weight, layer)
        if layer > 0:
            away = over_h(after(output[2], kept))
            output = [(a, 0) for a in (output[0], over_c(output[1]), away, diagonal)]
        ups = [(kept, None)] + [(r, None) for r in received]
        results[layer] = lax.dynamic_index_in_dim(
            sums.reshape(3, 4, width), clip, axis=1, keepdims=False
        )

    sums = jnp.stack(results)
    sums = [sums[:, 0], sums[:, 1], sums[:, 2]]
    away = merge(kept, 1, received[1], turn=1)
    later = (later[0], over_c(after(later[1], away)))
    come[0] = after(come[0], sums, later[1])
    away = over_h(away)
    near_sum, far_sum, near_go, far_go = step_of(
        (in_hbm(stay[0]), come[0]), (in_hbm(stay[1]), come[1]), cut=2
    )
    near_go, far_go = over_second(near_go), over_second(far_go)
    (go,) = step_of((far_sum, far_go), cut=0)
    (later,) = step_of(later, cut=0)
    later = four_of_plane(after(later, go, near_go))
    go = over_h(go)
    (total,) = step_of((near_sum, near_go), cut=0)
    output = unpack(place, [(after(array, total), i) for array, i in output], frames, waited=True)
    close = merge(kept, 0, after(received[0], output))
    far = over_c(after(away, received[0])[: 3 * frames // 2])
    (share,) = step_of((total, after(go, far, close, *later[1:])), cut=0)
    grad_in = [(close, 0), (over_c(close[frames:]), 0), (away, 1), (far, 0)]
    grad_in = unpack(place, grad_in, frames)
    grad_weights = assemble(place, after(later, grad_in), 1, by_core=False)
    gathered = plane_gather(share, grad_weights)
    grad_weights = assemble(place, gathered, 0, grad_weights)
    return (output, grad_in, grad_weights, *sums, sums[1])


def gelu_slope(value):
    return (
        0.5 * (1.0 + jax.scipy.special.erf(value / ROOT_TWO))
        + value * jnp.exp(-0.5 * value * value) / ROOT_TWO_PI
    )


def recur_step(decay, state, inputs):
    drive_t, valid_t = inputs
    pre = drive_t + decay * state
    state = state + valid_t * (jax.nn.gelu(pre, approximate=False) - state)
    return (state, state)


def back_step(decay, carry, inputs):
    upstream_t, valid_t, pre_t = inputs
    total = upstream_t + carry
    grad_pre = total * valid_t * gelu_slope(pre_t)
    carry = total * (1.0 - valid_t) + grad_pre * decay
    return (carry, grad_pre)


def add_piece(weight, piece):
    return jnp.dot(weight, piece, precision=HIGH, preferred_element_type=jnp.float32)


def weight_columns(grad_pre_norm, piece):
    return jnp.einsum("jf,kf->jk", grad_pre_norm, piece, precision=HIGH)


def split_features(inputs, weights, gains, shifts, decays, biases, lengths, frame_mask, grad_out):
    width, slots = inputs.shape
    clips, frames_len = frame_mask.shape
    frames = jnp.arange(frames_len, dtype=jnp.int32)
    valid_grid = (
        (frames[None, :] < lengths[:, None]) & ((frame_mask == 1) | (frames[None, :] == 0))
    ).astype(jnp.float32)
    valid = valid_grid.reshape(-1)
    valid_row = valid[None, :]
    valid_time = jnp.broadcast_to(valid_grid.T[:, :, None], (frames_len, clips, width)).reshape(
        frames_len, clips * width
    )
    count_local = jnp.sum(valid)

    def to_time(array):
        return jnp.transpose(array.reshape(width, clips, frames_len), (2, 1, 0)).reshape(
            frames_len, clips * width
        )

    def from_time(array):
        return jnp.transpose(array.reshape(frames_len, clips, width), (2, 1, 0)).reshape(
            width, slots
        )

    layer_in = inputs
    saved = []
    for layer_no in range(LAYERS):
        weight = weights[layer_no]
        gathered = lax.all_gather(layer_in, "neuron", axis=0, tiled=True)
        pre_norm = add_piece(weight, gathered)
        first_sum, count = lax.psum((jnp.sum(valid_row * pre_norm, axis=1), count_local), "batch")
        mean = first_sum / count
        centered = pre_norm - mean[:, None]
        var = lax.psum(jnp.sum(valid_row * centered * centered, axis=1), "batch") / count
        inv_std = lax.rsqrt(var + EPS)
        zhat = (pre_norm - mean[:, None]) * inv_std[:, None]
        drive = gains[layer_no][:, None] * zhat + (shifts[layer_no] + biases[layer_no])[:, None]
        drive_time = to_time(drive)
        decay_wide = jnp.tile(decays[layer_no], clips)
        start_state = jnp.zeros((clips * width,), jnp.float32)
        _, states = lax.scan(
            partial(recur_step, decay_wide), start_state, (drive_time, valid_time), unroll=8
        )
        saved.append((gathered, zhat, inv_std, drive_time, states, count))
        layer_in = layer_in + valid_row * from_time(states)
    upstream = grad_out
    grad_parts = [None] * LAYERS
    for layer_no in range(LAYERS - 1, -1, -1):
        gathered, zhat, inv_std, drive_time, states, count = saved[layer_no]
        decay_wide = jnp.tile(decays[layer_no], clips)
        gain = gains[layer_no]
        previous = jnp.concatenate([jnp.zeros_like(states[:1]), states[:-1]], axis=0)
        pre_time = drive_time + decay_wide[None, :] * previous
        grad_state = to_time(valid_row * upstream)
        start_carry = jnp.zeros((clips * width,), jnp.float32)
        _, grad_pre_time = lax.scan(
            partial(back_step, decay_wide),
            start_carry,
            (grad_state, valid_time, pre_time),
            reverse=True,
            unroll=8,
        )
        decay_local = jnp.sum(
            jnp.sum(grad_pre_time * previous, axis=0).reshape(clips, width), axis=0
        )
        grad_pre = from_time(grad_pre_time)
        gain_local = jnp.sum(grad_pre * zhat, axis=1)
        shift_local = jnp.sum(grad_pre, axis=1)
        grad_gain, grad_shift, grad_decay = lax.psum(
            (gain_local, shift_local, decay_local), "batch"
        )
        grad_pre_norm = (gain * inv_std)[:, None] * (
            grad_pre - valid_row * (grad_shift[:, None] + zhat * grad_gain[:, None]) / count
        )
        weight_local = weight_columns(grad_pre_norm, gathered)
        input_terms = jnp.einsum("jk,jf->kf", weights[layer_no], grad_pre_norm, precision=HIGH)
        input_grad = lax.psum_scatter(input_terms, "neuron", scatter_dimension=0, tiled=True)
        grad_weight = lax.psum(weight_local, "batch")
        upstream = upstream + input_grad
        grad_parts[layer_no] = (grad_weight, grad_gain, grad_shift, grad_decay)
    grad_weights = jnp.stack([grad_parts[layer_no][0] for layer_no in range(LAYERS)])
    grad_gains = jnp.stack([grad_parts[layer_no][1] for layer_no in range(LAYERS)])
    grad_shifts = jnp.stack([grad_parts[layer_no][2] for layer_no in range(LAYERS)])
    grad_decays = jnp.stack([grad_parts[layer_no][3] for layer_no in range(LAYERS)])
    return (layer_in, upstream, grad_weights, grad_gains, grad_shifts, grad_decays, grad_shifts)


def solution(mesh):
    if (mesh.shape["batch"], mesh.shape["neuron"]) == (4, 8):
        cut = Mesh(mesh.devices.reshape(2, 2, 2, 2, 2), ("y", "x", "h", "l", "c"))
        batch, neuron, body = ("y", "x"), ("h", "l", "c"), half_features
    else:
        cut, batch, neuron, body = mesh, "batch", "neuron", split_features
    in_specs = (
        P(neuron, batch),
        P(None, neuron, None),
        P(None, neuron),
        P(None, neuron),
        P(None, neuron),
        P(None, neuron),
        P(batch),
        P(batch, None),
        P(neuron, batch),
    )
    out_specs = (
        P(neuron, batch),
        P(neuron, batch),
        P(None, neuron, None),
        P(None, neuron),
        P(None, neuron),
        P(None, neuron),
        P(None, neuron),
    )
    return jax.shard_map(
        body, mesh=cut, in_specs=in_specs, out_specs=out_specs, check_vma=False
    )
```

```python
from functools import partial
import math

import jax
import jax.numpy as jnp
from jax import lax
from jax.experimental import pallas as pl
from jax.experimental.pallas import tpu as pltpu
from jax.sharding import Mesh, PartitionSpec as P

LAYERS = 2
EPS = 1e-05
HIGH = lax.Precision.HIGHEST
ROOT_TWO = math.sqrt(2.0)
ROOT_TWO_PI = math.sqrt(2.0 * math.pi)
F32 = jnp.float32
BF16 = jnp.bfloat16
LANES = 128
VMEM_LIMIT = 24 * 1024 * 1024
SMEM_SPEC = pl.BlockSpec(memory_space=pltpu.SMEM)
VMEM_SPEC = pl.BlockSpec(memory_space=pltpu.VMEM)


FLIP2 = [(0, 1), (1, 0)]
DIAGONAL = [(0, 3), (1, 2), (2, 1), (3, 0)]


def swap_half(array):
    return lax.ppermute(array, "l", FLIP2)


def after(value, *others):
    return lax.optimization_barrier((value, others))[0]


def split(value):
    high = value.astype(BF16)
    return high, (value - high.astype(F32)).astype(BF16)


def dot(a, b, dims):
    return lax.dot_general(a, b, (dims, ((), ())), preferred_element_type=F32)


NT = ((1,), (1,))
NN = ((1,), (0,))


def in_hbm(array):
    return pltpu.with_memory_space_constraint(array, pltpu.HBM)


def call(body, out_shape, hbm_outs=(), **kwargs):
    if hbm_outs:
        out_shape = [
            pltpu.HBM(a.shape, a.dtype) if i in hbm_outs else a for i, a in enumerate(out_shape)
        ]
    return pl.pallas_call(
        body,
        out_shape=out_shape,
        compiler_params=pltpu.CompilerParams(vmem_limit_bytes=VMEM_LIMIT),
        **kwargs,
    )


def cost(flops, byte_count):
    return pl.CostEstimate(flops=int(flops) // 64, bytes_accessed=int(byte_count) // 64, transcendentals=0)


def pack_body(frames, place_ref, in_ref, near_ref, far_ref, turned):
    slots = in_ref.shape[1]
    for start in range(0, slots, LANES):
        turned[start : start + LANES, :] = in_ref[:, start : start + LANES].T
    for rel in range(4):
        first = pl.multiple_of(place_ref[rel] * frames, 8)
        out = (near_ref, far_ref)[rel // 2]
        out[(rel % 2) * frames : (rel % 2 + 1) * frames, :] = turned[pl.ds(first, frames), :]


def pack(place, array, frames, waits=False):
    width, slots = array.shape
    out = jax.ShapeDtypeStruct((2 * frames, width), F32)
    return call(
        partial(pack_body, frames),
        grid=(1,),
        out_shape=[out, out],
        in_specs=[SMEM_SPEC, pl.BlockSpec((width, slots), lambda i: (0, 0))],
        out_specs=[pl.BlockSpec(out.shape, lambda i: (0, 0))] * 2,
        scratch_shapes=[pltpu.VMEM((slots, width), F32)],
        hbm_outs=(0, 1) if waits else (),
        cost_estimate=cost(0, 8 * width * slots),
        name="pack",
    )(place, in_hbm(array))


def part_spec(part, frames):
    array, i = part
    if i is None:
        return pl.BlockSpec(array.shape, lambda *_: (0,) * array.ndim)
    return pl.BlockSpec((frames, array.shape[1]), lambda *_: (i, 0))


def arrays_of(parts):
    return [array for array, _ in parts]


def unpack_body(frames, place_ref, *refs):
    ins, out_ref, turned = refs[:4], refs[4], refs[5]
    slots = out_ref.shape[1]
    for rel in range(4):
        first = pl.multiple_of(place_ref[rel] * frames, 8)
        turned[pl.ds(first, frames), :] = ins[rel][...]
    for start in range(0, slots, LANES):
        out_ref[:, start : start + LANES] = turned[start : start + LANES, :].T


def unpack(place, parts, frames, waited=False):
    width = parts[0][0].shape[1]
    slots = 4 * frames
    return call(
        partial(unpack_body, frames),
        grid=(1,),
        out_shape=jax.ShapeDtypeStruct((width, slots), F32),
        in_specs=[SMEM_SPEC] + [part_spec(part, frames) for part in parts],
        out_specs=pl.BlockSpec((width, slots), lambda i: (0, 0)),
        scratch_shapes=[pltpu.VMEM((slots, width), F32)],
        cost_estimate=cost(0, 8 * width * slots),
        name="unpack",
    )(place, *[in_hbm(a) if waited else a for a in arrays_of(parts)])


def merge_body(kept_ref, come_ref, *outs):
    frames, columns = kept_ref.shape
    width = columns // 2
    for i in range(2):
        some = slice(i * width, (i + 1) * width)
        if len(outs) > 1:
            outs[i][...] = kept_ref[:, some] + come_ref[:, some]
            continue
        (out_ref,) = outs
        out_ref[i * frames : (i + 1) * frames, :] = kept_ref[:, some] + come_ref[:, some]


def merge(kept, half, come, apart=False):
    frames, columns = come.shape
    rows, n = (frames, 2) if apart else (2 * frames, 1)
    outs = call(
        merge_body,
        grid=(1,),
        out_shape=[jax.ShapeDtypeStruct((rows, columns // 2), F32)] * n,
        in_specs=[
            pl.BlockSpec((frames, columns), lambda i: (0, half)),
            pl.BlockSpec((frames, columns), lambda i: (0, 0)),
        ],
        out_specs=[pl.BlockSpec((rows, columns // 2), lambda i: (0, 0))] * n,
        cost_estimate=cost(0, 12 * frames * columns),
        name="merge",
    )(kept, come)
    return outs if apart else outs[0]


def project_body(n_parts, n_flat, spots, n_weights, first, with_acc, with_stats, with_params, cols_ref, place_ref, *refs):
    del cols_ref

    def take(n):
        nonlocal refs
        some, refs = refs[:n], refs[n:]
        return some

    parts, flat_parts, weights = take(n_parts), take(n_flat), take(n_weights)
    acc, valid, stats_in, params = take(with_acc), take(with_stats > 0), take(with_stats > 1), take(with_params)
    (out_ref,) = take(1)
    stats, flat = take(with_stats > 0), take(n_flat > 0)
    x_high, x_low, far_ref = refs
    step = pl.program_id(0)
    width = x_high.shape[2]

    @pl.when(step == 0)
    def _():
        for block, part in zip(spots, parts):
            for start in range(0, part.shape[1], width):
                high, low = split(part[:, start : start + width])
                x_high[block + start // width] = high
                x_low[block + start // width] = low
        column = 0
        for part in flat_parts:
            flat[0][:, column : column + part.shape[1]] = part[...]
            column += part.shape[1]
        if with_acc:
            out_ref[...] = acc[0][...]
        else:
            out_ref[...] = jnp.zeros_like(out_ref)

    stacked = jnp.concatenate([x_high[step], x_low[step], x_high[step]], axis=1)
    for block, weight in enumerate(weight_blocks(place_ref, weights, far_ref)):
        w_high, w_low = split(weight)
        columns = slice(block * width, (block + 1) * width)
        out_ref[:, columns] += dot(stacked, jnp.concatenate([w_high, w_high, w_low], axis=1), NT)

    if with_stats:
        (stats_ref,) = stats

        @pl.when(step == pl.num_programs(0) - 1)
        def _():
            if stats_in:
                stats_ref[...] = stats_in[0][...]
            own = jnp.sum(valid[0][...], axis=0, keepdims=True)
            per = width // LANES
            for row in range(out_ref.shape[1] // LANES):
                z = out_ref[:, row * LANES : (row + 1) * LANES]
                total = jnp.sum(valid[0][...] * z, axis=0, keepdims=True)
                centred = valid[0][...] * (z - total / own)
                squares = jnp.sum(centred * centred, axis=0, keepdims=True)
                at = place_ref[first + row // per] * per + row % per
                stats_ref[0, pl.ds(at, 1), :] = total
                stats_ref[1, pl.ds(at, 1), :] = squares
                stats_ref[2, pl.ds(at, 1), :] = own
            if with_params:
                rest = params[0].shape[0] - 8
                stats_ref[3] = params[0][:8, :]
                stats_ref[4] = jnp.zeros_like(stats_ref[4])
                stats_ref[4, :rest, :] = params[0][8:, :]


def weight_specs(weights, layer, pairs=2):
    specs = []
    for weight in weights:
        if weight.ndim == 3:
            shape = (1, weight.shape[1], pairs * weight.shape[1])
            specs.append(pl.BlockSpec(shape, lambda s, cols, *_: (layer, 0, cols[s])))
        else:
            shape = (weight.shape[0], pairs * 4 * weight.shape[0])
            specs.append(pl.BlockSpec(shape, lambda s, cols, *_: (0, cols[s])))
    return specs


def far_scratch(width, pairs=2):
    return pltpu.VMEM((2, width, pairs * width), F32)


def weight_blocks(place_ref, refs, far_ref):
    near = [ref[0] for ref in refs if len(ref.shape) == 3]
    pieces = [ref for ref in refs if len(ref.shape) == 2]
    far = []
    for i in range(len(pieces) // 4):
        for rel, piece in enumerate(pieces[4 * i : 4 * i + 4]):
            rows = piece.shape[0]
            row = 2 * (place_ref[4] ^ (rel // 2)) + (place_ref[5] ^ (rel % 2))
            far_ref[i, pl.ds(pl.multiple_of(row * rows, rows), rows), :] = piece[...]
        far.append(far_ref[i])
    return near + far


def project(
    place, frames, parts, blocks, weights, layer, acc=None, valid=None, stats=None, params=None, flat=()
):
    near = weights[0].ndim == 3
    units = sum(1 if w.ndim == 3 else 0.25 for w in weights)
    width = weights[0].shape[1] if near else 4 * weights[0].shape[0]
    n = blocks.shape[0]
    spots, block = [], 0
    for array, _ in parts:
        spots.append(block)
        block += array.shape[1] // width
    full = pl.BlockSpec(memory_space=pltpu.VMEM)
    in_specs = [part_spec(part, frames) for part in (*parts, *flat)]
    in_specs += weight_specs(weights, layer, 1)
    operands = arrays_of(parts) + arrays_of(flat) + [in_hbm(w) for w in weights]
    array = jax.ShapeDtypeStruct((frames, int(units) * width), F32)
    array_spec = pl.BlockSpec(array.shape, lambda s, cols, place: (0, 0))
    out_shape, out_specs = [array], [array_spec]
    if acc is not None:
        in_specs.append(array_spec)
        operands.append(in_hbm(acc))
    if valid is not None:
        in_specs.append(full)
        operands.append(valid)
        shape = (3 if params is None else 5, 4 * width // LANES, LANES)
        out_shape.append(jax.ShapeDtypeStruct(shape, F32))
        out_specs.append(pl.BlockSpec(shape, lambda s, cols, place: (0, 0, 0)))
    for extra in (stats, params):
        if extra is not None:
            in_specs.append(full)
            operands.append(extra)
    if flat:
        out_shape.append(jax.ShapeDtypeStruct((frames, 4 * width), F32))
        out_specs.append(pl.BlockSpec((frames, 4 * width), lambda s, cols, place: (0, 0)))
    return call(
        partial(
            project_body,
            len(parts),
            len(flat),
            spots,
            len(weights),
            0 if near else 2,
            acc is not None,
            (valid is not None) + (stats is not None),
            params is not None,
        ),
        grid_spec=pltpu.PrefetchScalarGridSpec(
            num_scalar_prefetch=2,
            grid=(n,),
            in_specs=in_specs,
            out_specs=out_specs,
            scratch_shapes=[pltpu.VMEM((n, frames, width), BF16)] * 2 + [far_scratch(width, 1)],
        ),
        out_shape=out_shape,
        hbm_outs=(0, len(out_shape) - 1) if flat else (0,),
        cost_estimate=cost(6 * frames * n * width * units * width, 4 * n * width * units * width),
        name="project",
    )(blocks, place, *operands)


def to_relative(place_ref, spread, rows_ref, value, slot):
    per = value.shape[0] // 4
    spread[...] = value
    for rel in range(4):
        first = place_ref[rel] * per
        for row in range(per):
            rows_ref[slot, rel * per + row : rel * per + row + 1, :] = spread[
                pl.ds(first + row, 1), :
            ]


def tree(values):
    while len(values) > 1:
        values = [a + b for a, b in zip(values[::2], values[1::2])]
    return values[0]


def gathered(ref, slot):
    return [ref[i] for i in range(slot, ref.shape[0], ref.shape[0] // 16)]


def norm_terms(stats_ref):
    each = [gathered(stats_ref, slot) for slot in range(3)]
    totals, squares, owns = each
    count = tree(owns)
    mean = tree(totals) / count
    away = [total / own - mean for total, own in zip(totals, owns)]
    spread = tree([s + n * a * a for s, n, a in zip(squares, owns, away)])
    return count, mean, lax.rsqrt(spread / count + EPS)


CHUNKS = 4


def columns_of(refs, row):
    for ref in refs:
        if row * LANES < ref.shape[1]:
            return ref[:, row * LANES : (row + 1) * LANES]
        row -= ref.shape[1] // LANES


def recur_body(n_z, last, layer, spread_params, place_ref, gate_ref, *refs):
    z_refs, refs = refs[:n_z], refs[n_z:]
    (stats_ref, params_ref, valid_ref, x_ref), refs = refs[:4], refs[4:]
    outs, refs = refs[: 1 + 3 * last], refs[1 + 3 * last :]
    if spread_params:
        state_ref, slope_ref, params_out, rows, spread, held, drive_s, state_s, slope_s = refs
    else:
        state_ref, slope_ref, rows, spread, held, drive_s, state_s, slope_s = refs
    frames, features = x_ref.shape
    blocks = features // LANES
    per = blocks // 4
    chunk = pl.program_id(0)

    @pl.when(chunk == 0)
    def _():
        if spread_params:
            for rel in range(4):
                first = place_ref[rel] * (stats_ref.shape[0] // 16) + 3
                for row in range(LAYERS * 3 * per):
                    at = rel * per + row % per
                    params_out[row // per, at : at + 1, :] = stats_ref[
                        first + row // 8, row % 8 : row % 8 + 1, :
                    ]
            params = [params_out[3 * layer + i] for i in range(3)]
        else:
            params = [params_ref[3 * layer + i] for i in range(3)]
        _, mean, inv_std = norm_terms(stats_ref)
        to_relative(place_ref, spread, rows, mean, 0)
        to_relative(place_ref, spread, rows, inv_std, 1)
        rows[1] = rows[1] * params[0]
        rows[2] = params[1]
        rows[3] = params[2]
        held[...] = jnp.zeros_like(held)

    for row in range(blocks):
        drive_s[row * frames : (row + 1) * frames, :] = (
            columns_of(z_refs, row) - rows[0, row : row + 1, :]
        ) * rows[1, row : row + 1, :] + rows[2, row : row + 1, :]
    decay = rows[3]

    def step(t, state):
        at = pl.ds(t, blocks, stride=frames)
        pre = drive_s[at, :] + decay * state
        half = 0.5 + 0.5 * lax.erf(pre * (1.0 / ROOT_TWO))
        gate = gate_ref[chunk * frames + t] > 0.0
        slope = half + pre * jnp.exp(-0.5 * pre * pre) * (1.0 / ROOT_TWO_PI)
        state = jnp.where(gate, pre * half, state)
        state_s[at, :] = state
        slope_s[at, :] = jnp.where(gate, slope, 0.0)
        return state

    held[...] = lax.fori_loop(0, frames, step, held[...], unroll=8)
    valid = valid_ref[...]
    for row in range(blocks):
        lanes = slice(row * LANES, (row + 1) * LANES)
        state = state_s[row * frames : (row + 1) * frames, :]
        state_ref[:, lanes] = state
        slope_ref[:, lanes] = slope_s[row * frames : (row + 1) * frames, :]
        value = x_ref[:, lanes] + valid * state
        out, at = (outs[row // per], row % per) if last else (outs[0], row)
        out[:, at * LANES : (at + 1) * LANES] = value


def recur(layer, place, gate, z, stats, params, valid, x, last):
    frames, features = x.shape
    blocks = features // LANES
    some = frames // CHUNKS
    whole = lambda array: pl.BlockSpec(array.shape, lambda i: (0,) * array.ndim)
    by_chunk = lambda array: pl.BlockSpec((some, array.shape[1]), lambda i: (i, 0))
    full = jax.ShapeDtypeStruct((frames, features), F32)
    piece = jax.ShapeDtypeStruct((frames, features // 4), F32)
    out_shape = [piece] * 4 if last else [full]
    out_shape += [full, full]
    out_specs = [by_chunk(a) for a in out_shape]
    spread_params = params is None
    if spread_params:
        out_shape.append(jax.ShapeDtypeStruct((3 * LAYERS, blocks, LANES), F32))
        out_specs.append(whole(out_shape[-1]))
        params = valid
    return call(
        partial(recur_body, len(z), last, layer, spread_params),
        grid=(CHUNKS,),
        in_specs=[SMEM_SPEC, SMEM_SPEC]
        + [by_chunk(a) for a in z]
        + [whole(a) for a in (stats, params)]
        + [by_chunk(a) for a in (valid, x)],
        out_specs=out_specs,
        out_shape=out_shape,
        hbm_outs=tuple(range(len(out_shape) - spread_params)) if last else (1, 2),
        scratch_shapes=[
            pltpu.VMEM((4, blocks, LANES), F32),
            pltpu.VMEM((blocks, LANES), F32),
            pltpu.VMEM((blocks, LANES), F32),
        ]
        + [pltpu.VMEM((blocks * some, LANES), F32)] * 3,
        cost_estimate=cost(100 * frames * features, 20 * frames * features),
        name="recur",
    )(place, gate, *[in_hbm(a) for a in z], stats, params, valid, in_hbm(x))


def back_body(n_z, n_ups, spots, layer, place_ref, gate_ref, *refs):
    z_refs, refs = refs[:n_z], refs[n_z:]
    (stats_ref, params_ref), refs = refs[:2], refs[2:]
    ups, (state_ref, slope_ref), refs = refs[:n_ups], refs[n_ups : n_ups + 2], refs[n_ups + 2 :]
    grad_ref, sums_ref, rows, spread, held, up_s, state_s, slope_s = refs
    frames, features = state_ref.shape
    blocks = features // LANES
    per = blocks // 4
    tall = frames + 8
    step_no = pl.program_id(0)
    chunk = pl.num_programs(0) - 1 - step_no

    @pl.when(step_no == 0)
    def _():
        _, mean, inv_std = norm_terms(stats_ref)
        to_relative(place_ref, spread, rows, mean, 0)
        to_relative(place_ref, spread, rows, inv_std, 1)
        held[...] = jnp.zeros_like(held)

    for row in range(blocks):
        lanes = slice(row * LANES, (row + 1) * LANES)
        base = row * frames
        up = None
        for (_, column), part in zip(spots, ups):
            if column <= row * LANES < column + part.shape[1]:
                value = part[:, row * LANES - column : (row + 1) * LANES - column]
                up = value if up is None else up + value
        up_s[base : base + frames, :] = up
        state_s[row * tall : row * tall + 8, :] = jnp.zeros((8, LANES), F32)
        state_s[row * tall + 8 : (row + 1) * tall, :] = state_ref[:, lanes]
        slope_s[base : base + frames, :] = slope_ref[:, lanes]
    decay = params_ref[3 * layer + 2]

    def step(i, carry):
        t = frames - 1 - i
        at = pl.ds(t, blocks, stride=frames)
        slope = slope_s[at, :]
        gate = gate_ref[chunk * frames + t]
        total = gate * up_s[at, :] + carry
        up_s[at, :] = total * slope
        return total * (slope * decay + (1.0 - gate))

    held[0] = lax.fori_loop(0, frames, step, held[0], unroll=8)
    held[4] += held[1] * state_s[pl.ds(tall - 1, blocks, stride=tall), :]
    held[1] = up_s[pl.ds(0, blocks, stride=frames), :]
    for row in range(blocks):
        lanes = slice(row * LANES, (row + 1) * LANES)
        grad = up_s[row * frames : (row + 1) * frames, :]
        grad_ref[:, lanes] = grad
        zhat = (columns_of(z_refs, row) - rows[0, row : row + 1, :]) * rows[1, row : row + 1, :]
        before = state_s[row * tall + 7 : row * tall + 7 + frames, :]
        for slot, value in enumerate((grad * zhat, grad, grad * before)):
            held[2 + slot, row : row + 1, :] += jnp.sum(value, axis=0, keepdims=True)

    @pl.when(chunk == 0)
    def _():
        for row in range(blocks):
            at = place_ref[row // per] * per + row % per
            for slot in range(3):
                sums_ref[slot, pl.ds(at, 1), :] = held[2 + slot, row : row + 1, :]


def spots_of_sum(parts, width):
    spots, column = [], 0
    for array, _ in parts:
        spots.append((0, column % (4 * width)))
        column += array.shape[1]
    return spots


def back(layer, place, gate, z, stats, params, ups, states, slopes):
    frames, features = states.shape
    width = features // 4
    blocks = features // LANES
    some = frames // CHUNKS
    whole = lambda array: pl.BlockSpec(array.shape, lambda i: (0,) * array.ndim)

    def by_chunk(array, first=0):
        return pl.BlockSpec(
            (some, array.shape[1]), lambda i: ((first or 0) * CHUNKS + CHUNKS - 1 - i, 0)
        )

    out_shape = [
        jax.ShapeDtypeStruct((frames, features), F32),
        jax.ShapeDtypeStruct((3, blocks, LANES), F32),
    ]
    return call(
        partial(back_body, len(z), len(ups), spots_of_sum(ups, width), layer),
        grid=(CHUNKS,),
        in_specs=[SMEM_SPEC] * 2
        + [by_chunk(a) for a in z]
        + [whole(a) for a in (stats, params)]
        + [by_chunk(*up) for up in ups]
        + [by_chunk(a) for a in (states, slopes)],
        out_specs=[by_chunk(out_shape[0]), whole(out_shape[1])],
        out_shape=out_shape,
        scratch_shapes=[
            pltpu.VMEM((2, blocks, LANES), F32),
            pltpu.VMEM((blocks, LANES), F32),
            pltpu.VMEM((5, blocks, LANES), F32),
            pltpu.VMEM((blocks * some, LANES), F32),
            pltpu.VMEM((blocks * (some + 8), LANES), F32),
            pltpu.VMEM((blocks * some, LANES), F32),
        ],
        cost_estimate=cost(30 * frames * features, 20 * frames * features),
        name="back",
    )(
        place,
        gate,
        *[in_hbm(a) for a in z],
        stats,
        params,
        *arrays_of(ups),
        in_hbm(states),
        in_hbm(slopes),
    )


def input_terms(high_s, low_s, weights):
    left, right = [], []
    for block, weight in enumerate(weights):
        w_high, w_low = split(weight)
        left += [high_s[block], low_s[block], high_s[block]]
        right += [w_high, w_high, w_low]
    return dot(jnp.concatenate(left, axis=1), jnp.concatenate(right, axis=0), NN)


def norm_back_body(n_z, split_terms, layer, cols_ref, place_ref, grad_ref, *refs):
    del cols_ref
    z_refs, refs = refs[:n_z], refs[n_z:]
    params_ref, valid_ref, stats_ref, sums_ref, *refs = refs
    weights, refs = refs[:10], refs[10:]
    if split_terms:
        out_ref, leave_ref, near_term_ref, far_term_ref, sums_out_ref, *refs = refs
        term_refs, starts = (far_term_ref, near_term_ref), (0, 0)
    else:
        out_ref, leave_ref, term_ref, sums_out_ref, *refs = refs
        term_refs, starts = (term_ref, term_ref), (2 * grad_ref.shape[1] // 4, 0)
    rows, spread, high_s, low_s, far_ref = refs
    blocks = grad_ref.shape[1] // LANES
    width = high_s.shape[2]
    per = width // LANES

    @pl.when(pl.program_id(0) == 0)
    def _():
        count, mean, inv_std = norm_terms(stats_ref)
        to_relative(place_ref, spread, rows, mean, 0)
        to_relative(place_ref, spread, rows, inv_std, 1)
        rows[2] = rows[1] * params_ref[3 * layer]
        sums = [tree(gathered(sums_ref, slot)) for slot in range(3)]
        for slot in range(3):
            sums_out_ref[slot] = sums[slot]
        to_relative(place_ref, spread, rows, sums[0] / count, 3)
        to_relative(place_ref, spread, rows, sums[1] / count, 4)
        valid = valid_ref[...]
        for row in range(blocks):
            lanes = slice(row * LANES, (row + 1) * LANES)
            one = lambda slot: rows[slot, row : row + 1, :]
            zhat = (columns_of(z_refs, row) - one(0)) * one(1)
            value = one(2) * (grad_ref[:, lanes] - valid * (one(4) + zhat * one(3)))
            out_ref[:, lanes] = value
            if (row // per) % 2:
                at = (row // per // 2) * width + (row % per) * LANES
                leave_ref[:, at : at + LANES] = value
            high, low = split(value)
            inner = slice((row % per) * LANES, (row % per + 1) * LANES)
            high_s[row // per, :, inner] = high
            low_s[row // per, :, inner] = low

    value = input_terms(high_s, low_s, weight_blocks(place_ref, weights, far_ref))
    for step, (term_ref, first) in enumerate(zip(term_refs, starts)):

        @pl.when(pl.program_id(0) == step)
        def _():
            for pair in range(2):
                at = pl.multiple_of(((place_ref[0] & 1) ^ pair) * width, width)
                term_ref[:, pl.ds(first + at, width)] = value[
                    :, pair * width : (pair + 1) * width
                ]


def norm_back(columns, place, grad, z, params, valid, stats, sums, weights, layer, split_terms):
    frames, features = grad.shape
    width = features // 4
    blocks = features // LANES
    whole = lambda array: pl.BlockSpec(array.shape, lambda s, cols, place: (0,) * array.ndim)
    operands = [grad, *[in_hbm(a) for a in z], params, valid, stats, sums]
    full = jax.ShapeDtypeStruct((frames, features), F32)
    half = jax.ShapeDtypeStruct((frames, 2 * width), F32)
    terms = [half, half] if split_terms else [full]
    out_shape = [full, half, *terms, jax.ShapeDtypeStruct((3, blocks, LANES), F32)]
    return call(
        partial(norm_back_body, len(z), split_terms, layer),
        grid_spec=pltpu.PrefetchScalarGridSpec(
            num_scalar_prefetch=2,
            grid=(2,),
            in_specs=[whole(a) for a in operands] + weight_specs(weights, layer),
            out_specs=[whole(a) for a in out_shape],
            scratch_shapes=[
                pltpu.VMEM((5, blocks, LANES), F32),
                pltpu.VMEM((blocks, LANES), F32),
                pltpu.VMEM((4, frames, width), BF16),
                pltpu.VMEM((4, frames, width), BF16),
                far_scratch(width),
            ],
        ),
        out_shape=out_shape,
        hbm_outs=(0,),
        cost_estimate=cost(6 * frames * features * features, 4 * features * features),
        name="norm_back",
    )(columns, place, *operands, *[in_hbm(w) for w in weights])


def own_terms_body(n_ups, spots, cols_ref, place_ref, grad_ref, *refs):
    del cols_ref
    ups, refs = refs[:n_ups], refs[n_ups:]
    weights, refs = refs[:10], refs[10:]
    out_ref, high_s, low_s, far_ref = refs
    width = high_s.shape[2]
    step = pl.program_id(0)

    @pl.when(step == 0)
    def _():
        for block in range(4):
            high, low = split(grad_ref[:, block * width : (block + 1) * width])
            high_s[block] = high
            low_s[block] = low

    value = input_terms(high_s, low_s, weight_blocks(place_ref, weights, far_ref))
    for pair in range(2):
        at = pl.multiple_of(((place_ref[0] & 1) ^ pair) * width, width)
        out_ref[:, pl.ds(at, width)] = value[:, pair * width : (pair + 1) * width]
    for half in range(2):

        @pl.when(step == half)
        def _():
            first = 2 * half * width
            for (_, column), up in zip(spots, ups):
                low = max(column, first)
                high = min(column + up.shape[1], first + 2 * width)
                if low < high:
                    out_ref[:, low - first : high - first] += up[:, low - column : high - column]


def own_terms(columns, place, grad, ups, weights, layer):
    frames, features = grad.shape
    width = features // 4
    whole = lambda array: pl.BlockSpec(array.shape, lambda s, cols, place: (0,) * array.ndim)
    step_block = pl.BlockSpec((frames, 2 * width), lambda s, cols, place: (0, s))
    return call(
        partial(own_terms_body, len(ups), spots_of_sum(ups, width)),
        grid_spec=pltpu.PrefetchScalarGridSpec(
            num_scalar_prefetch=2,
            grid=(2,),
            in_specs=[whole(grad)]
            + [part_spec(up, frames) for up in ups]
            + weight_specs(weights, layer),
            out_specs=step_block,
            scratch_shapes=[pltpu.VMEM((4, frames, width), BF16)] * 2 + [far_scratch(width)],
        ),
        out_shape=jax.ShapeDtypeStruct((frames, features), F32),
        cost_estimate=cost(6 * frames * features * features, 4 * features * features),
        name="own_terms",
    )(columns, place, in_hbm(grad), *arrays_of(ups), *[in_hbm(w) for w in weights])


def prepare_body(lists_ref, place_ref, own_ref, near_ref, high_ref, low_ref):
    del lists_ref
    padded = high_ref.shape[0] // 2
    width = high_ref.shape[1] // 2
    for clip, part in enumerate((own_ref, near_ref)):
        rows = part.shape[0]
        for dc in range(2):
            at = pl.multiple_of((place_ref[6] ^ clip ^ dc) * width, width)
            high, low = split(part[:, dc * width : (dc + 1) * width])
            high_ref[clip * padded : clip * padded + rows, pl.ds(at, width)] = high
            low_ref[clip * padded : clip * padded + rows, pl.ds(at, width)] = low
        zeros = jnp.zeros((padded - rows, 2 * width), BF16)
        high_ref[clip * padded + rows : (clip + 1) * padded, :] = zeros
        low_ref[clip * padded + rows : (clip + 1) * padded, :] = zeros


def prepare(place, own, near):
    frames, features = own.shape
    width = features // 4
    padded = -(-frames // LANES) * LANES
    in_spec = pl.BlockSpec((frames, 2 * width), lambda s, *_: (0, s))
    out = jax.ShapeDtypeStruct((2 * padded, features), BF16)
    out_spec = pl.BlockSpec((2 * padded, 2 * width), lambda s, order, place: (0, order[s]))
    order = jnp.stack([place[0] >> 1, 1 - (place[0] >> 1)])
    return call(
        prepare_body,
        grid_spec=pltpu.PrefetchScalarGridSpec(
            num_scalar_prefetch=2,
            grid=(2,),
            in_specs=[in_spec, in_spec],
            out_specs=[out_spec, out_spec],
        ),
        out_shape=[out, out],
        hbm_outs=(0, 1),
        cost_estimate=cost(0, 16 * frames * features),
        name="prepare",
    )(order, place, in_hbm(own), in_hbm(near))


def product(g_high, g_low, x_high, x_low):
    return dot(g_high, x_high, NN) + (dot(g_high, x_low, NN) + dot(g_low, x_high, NN))


def weight_body(turn, place_ref, *refs):
    if turn:
        grad_ref, near_ref, x_high, x_low, kept, sent, g_high, g_low, t_high, t_low = refs

        @pl.when(pl.program_id(0) == 0)
        def _():
            frames, features = grad_ref.shape
            width = features // 4
            rows = width // 4
            padded = t_high.shape[1] // 2
            t_high[...] = jnp.zeros_like(t_high)
            t_low[...] = jnp.zeros_like(t_low)
            for clip in range(2):
                for dh in range(2):
                    if clip == 0:
                        part = grad_ref[:, 2 * dh * width : (2 * dh + 1) * width]
                    else:
                        part = near_ref[:, dh * width : (dh + 1) * width]
                    high, low = split(part.T)
                    at = (
                        slice(dh * width, (dh + 1) * width),
                        slice(clip * padded, clip * padded + frames),
                    )
                    t_high[at] = high
                    t_low[at] = low
            for group in range(8):
                first, second, dh = group // 4, group // 2 % 2, group % 2
                core = place_ref[6]
                y = place_ref[4] ^ (first * core + second * (1 - core))
                x = place_ref[5] ^ (first * (1 - core) + second * core)
                at = pl.multiple_of(dh * width + (2 * y + x) * rows, rows)
                g_high[group * rows : (group + 1) * rows, :] = t_high[pl.ds(at, rows), :]
                g_low[group * rows : (group + 1) * rows, :] = t_low[pl.ds(at, rows), :]

    else:
        g_high, g_low, x_high, x_low, kept, sent = refs
    half = g_high.shape[0] // 2
    value = product(g_high[...], g_low[...], x_high[...], x_low[...])
    kept[...] = value[:half].reshape(kept.shape)
    sent[...] = value[half:].reshape(sent.shape)


def weight_rows(side, place, grads, x_split, width):
    turn = side == 0
    whole = lambda array: pl.BlockSpec(array.shape, lambda s, place: (0,) * array.ndim)
    x_spec = pl.BlockSpec((x_split[0].shape[0], width), lambda s, place: (0, s))
    shape = (2, 2, width // 4, 4 * width)
    out_shape = [jax.ShapeDtypeStruct(shape, F32)] * 2
    out_specs = [pl.BlockSpec(shape[:3] + (width,), lambda s, place: (0, 0, 0, s))] * 2
    scratch = []
    if turn:
        turned = (2 * width, x_split[0].shape[0])
        out_shape += [jax.ShapeDtypeStruct(turned, BF16)] * 2
        out_specs += [whole(out_shape[-1])] * 2
        scratch = [pltpu.VMEM(turned, BF16)] * 2
    return call(
        partial(weight_body, turn),
        grid_spec=pltpu.PrefetchScalarGridSpec(
            num_scalar_prefetch=1,
            grid=(4,),
            in_specs=[whole(a) for a in grads] + [x_spec] * 2,
            out_specs=out_specs,
            scratch_shapes=scratch,
        ),
        out_shape=out_shape,
        hbm_outs=(0,),
        cost_estimate=cost(12 * x_split[0].shape[0] * width * 4 * width, 4 * 8 * width * width),
        name="weight_rows",
    )(place, *([in_hbm(grads[0]), grads[1]] if turn else grads), *[in_hbm(x) for x in x_split])


def step_body(n, widths, cut, *refs):
    ins, outs = refs[: 2 * n], refs[2 * n :]
    starts = [sum(widths[:i]) for i in range(len(widths))]
    column = 0
    for i in range(n):
        total = ins[2 * i][...] + ins[2 * i + 1][...]
        end = column + total.shape[-1]
        for j, (start, columns) in enumerate(zip(starts, widths)):
            low, high = max(start, column), min(start + columns, end)
            if low < high:
                to = (Ellipsis, slice(low - start, high - start))
                piece = total[..., low - column : high - column]
                pieces = [piece]
                for _ in range(cut):
                    pieces = [half[k] for half in pieces for k in range(2)]
                for k, some in enumerate(pieces):
                    outs[len(pieces) * j + k][to] = some
        column = end


def step_of(*pairs, cut=1, widths=None):
    shape = list(pairs[0][0].shape)
    widths = widths or [sum(pair[0].shape[-1] for pair in pairs)]
    outs = []
    for columns in widths:
        shape[-1] = columns
        outs += [jax.ShapeDtypeStruct(tuple(shape[cut:]), F32)] * 2**cut
    whole = lambda array: pl.BlockSpec(array.shape, lambda i: (0,) * array.ndim)
    operands = [array for pair in pairs for array in pair]
    return call(
        partial(step_body, len(pairs), widths, cut),
        grid=(1,),
        in_specs=[whole(a) for a in operands],
        out_specs=[whole(a) for a in outs],
        out_shape=outs,
        cost_estimate=cost(0, 4 * sum(a.size for a in operands)),
        name="reduction_step",
    )(*operands)


def plane_swap(array, step):
    pairs = []
    for i in range(8):
        over_x = (i % 2 == 0) == (step == 0)
        pairs.append((i, i ^ 2 if over_x else i ^ 4))
    return lax.ppermute(array, ("y", "x", "c"), pairs)


def plane_gather(share, *before):
    first = plane_swap(share, 0)
    second = plane_swap(share, 1)
    return [share, second, first, plane_swap(after(first, second, *before), 1)]


def assemble_body(place_ref, *refs):
    out_ref = refs[-1]
    core = place_ref[6]
    rows, columns = refs[0].shape
    quarter = columns // 4
    for i in range(4):
        first, second = i // 2, i % 2
        y = place_ref[4] ^ (first * core + second * (1 - core))
        x = place_ref[5] ^ (first * (1 - core) + second * core)
        at = pl.multiple_of((2 * y + x) * rows, rows)
        for side in range(2):
            for h in range(2):
                to = pl.multiple_of((2 * h + (place_ref[7] ^ side)) * quarter, quarter)
                some = slice((2 * side + h) * quarter, (2 * side + h + 1) * quarter)
                out_ref[0, pl.ds(at, rows), pl.ds(to, quarter)] = refs[i][:, some]


def assemble(place, pieces, layer, onto=None):
    rows, columns = 4 * pieces[0].shape[0], pieces[0].shape[1]
    aliases, extra, extra_specs = {}, [], []
    if onto is not None:
        aliases, extra = {1 + len(pieces): 0}, [onto]
        extra_specs = [pl.BlockSpec(memory_space=pl.ANY)]
    (out,) = call(
        assemble_body,
        grid=(1,),
        out_shape=[jax.ShapeDtypeStruct((LAYERS, rows, columns), F32)],
        hbm_outs=(0,),
        in_specs=[SMEM_SPEC]
        + [pl.BlockSpec(p.shape, lambda i: (0, 0)) for p in pieces]
        + extra_specs,
        out_specs=[pl.BlockSpec((1, rows, columns), lambda i: (layer, 0, 0))],
        input_output_aliases=aliases,
        cost_estimate=cost(0, 8 * rows * columns),
        name="assemble",
    )(place, *[p if extra else in_hbm(p) for p in pieces], *extra)
    return out


def half_features(inputs, weights, gains, shifts, decays, biases, lengths, frame_mask, grad_out):
    width, slots = inputs.shape
    clips, frames = frame_mask.shape
    depth = weights.shape[2]
    blocks = 4 * width // LANES
    y, x, h, l, c = (lax.axis_index(name) for name in ("y", "x", "h", "l", "c"))
    b = 2 * y + x
    numbers = [2 * (h ^ (rel // 2)) + (c ^ (rel % 2)) for rel in range(4)] + [y, x, c, l]
    place = jnp.stack(numbers).astype(jnp.int32)
    own_blocks, other_blocks = (
        jnp.stack(
            [2 * (2 * (h ^ (rel // 2)) + half) + (c ^ (rel % 2)) for rel in range(4)]
        ).astype(jnp.int32)
        for half in (l, 1 - l)
    )
    own_columns = jnp.stack([2 * h + l, 2 * (1 - h) + l]).astype(jnp.int32)
    other_columns = jnp.stack([2 * (1 - h) + 1 - l, 2 * h + 1 - l]).astype(jnp.int32)
    rows = width // 4

    clip = 2 * h + c
    seen = lax.dynamic_index_in_dim(frame_mask, clip, 0, keepdims=False)
    length = lax.dynamic_index_in_dim(lengths, clip, 0, keepdims=False)
    moments = jnp.arange(frames, dtype=jnp.int32)
    gate = ((moments < length) & ((seen == 1) | (moments == 0))).astype(F32)
    valid = jnp.broadcast_to(gate[:, None], (frames, LANES))

    def far_share(layer):
        return lax.dynamic_slice(weights, (layer, b * rows, 0), (1, rows, depth))[0]

    def over_h(array):
        return lax.ppermute(array, "h", FLIP2)

    def over_c(array):
        return lax.ppermute(array, "c", FLIP2)

    def over_second(array):
        return plane_swap(array, 1)

    def four_of(near_rows, far_rows):
        return [
            (near_rows, 0),
            (over_c(near_rows), 1),
            (far_rows, 0),
            (over_c(far_rows), 1),
        ]

    def four_of_plane(share):
        both = lax.ppermute(share, ("y", "x"), DIAGONAL)
        return [share, lax.ppermute(share, "x", FLIP2), lax.ppermute(share, "y", FLIP2), both]

    near = over_c(weights)
    share = far_share(0)
    close, away = pack(place, after(inputs, share), frames)
    share = over_h(share)
    away = over_h(away)
    other_close = swap_half(close)
    up_close, up_away = pack(place, after(grad_out, close), frames, waits=True)
    share = after(share, up_close, valid, near, other_close)
    pieces = four_of_plane(share)
    away = after(away, pieces[1:])
    half_weights = [[weights, near, *pieces, *map(over_c, after(pieces, away))]]
    own = four_of(after(close, away), away)
    other_away = swap_half(away)
    others = [(other_close, 0), (over_c(other_close), 1)]
    params = jnp.stack([gains, shifts + biases, decays], axis=1)
    own_params = params.reshape(LAYERS * 3 * width // LANES, LANES)
    params = None

    def gather(array, axes):
        return lax.all_gather(array, axes, tiled=True)

    weight = half_weights[0]
    early = jnp.concatenate([own_blocks, other_blocks[:2]])
    z, own_flat = project(place, frames, own + others, early, weight, 0, flat=own)
    others += [(other_away, 0), (over_c(after(other_away, z)), 1)]
    z, stats, other_flat = project(
        place,
        frames,
        others[2:],
        other_blocks[2:],
        weight,
        0,
        z,
        valid,
        params=own_params,
        flat=others,
    )
    z = [z]
    stats = gather(stats, ("h", "c"))
    share = over_c(lax.ppermute(after(far_share(1), stats), ("h", "c"), DIAGONAL))
    stats = gather(stats, ("y", "x"))
    x, states, slopes, params = recur(0, place, gate, z, stats, None, valid, own_flat, False)
    own_near, other_near = over_c(after(own_flat, z[0])), over_c(after(other_flat, z[0]))
    x_near = over_c(x)
    own_split = prepare(place, after(own_flat, x_near), own_near)
    other_split = prepare(place, after(other_flat, x_near), other_near)
    saved = [(own_split, other_split, z, stats, states, slopes)]

    pieces = four_of_plane(after(share, slopes, own_near, other_near))
    near = [weights, near]
    other = swap_half(x)
    x_own = after(x, own_split[0], other_split[0])
    z, *_ = project(place, frames, [(x_own, None)], own_blocks, near, 1)
    own_split = prepare(place, after(x, z), x_near)
    far = [*pieces, *map(over_c, after(pieces, own_split[0]))]
    up_away = over_h(after(up_away, other, own_split[0]))
    half_weights.append(near + far)
    z, stats = project(place, frames, [(other, None)], other_blocks, near, 1, z, valid)
    both = jnp.concatenate([own_blocks, other_blocks])
    z_far, stats = project(
        place,
        frames,
        [(x, None), (other, None)],
        both,
        far,
        1,
        None,
        valid,
        stats,
    )
    z = [z, z_far]
    stats = gather(gather(stats, ("y", "x")), ("h", "c"))
    upstream = four_of(up_close, after(up_away, stats))
    *output, states, slopes = recur(1, place, gate, z, stats, params, valid, x, True)
    other_near = over_c(after(other, slopes))
    saved.append((own_split, (other, other_near), z, stats, states, slopes))
    diagonal = over_c(over_h(output[3]))

    ups = upstream
    results = [None] * LAYERS
    for layer in range(LAYERS - 1, -1, -1):
        own_split, other_split, z, stats, states, slopes = saved[layer]
        weight = half_weights[layer]
        grad_pre, sums = back(layer, place, gate, z, stats, params, ups, states, slopes)
        sums = gather(sums, ("y", "x"))
        if layer == 0:
            come[0] = after(come[0], sums, away, output[1][0])
            later, go = step_of((in_hbm(stay[0]), come[0]), (in_hbm(stay[1]), come[1]))
            sums = after(sums, later)
            go = over_second(go)
        sums = gather(sums, ("h", "c"))
        grad_z, leaving, *terms, sums = norm_back(
            other_columns, place, grad_pre, z, params, valid, stats, sums, weight, layer,
            layer == 0,
        )
        leaving = over_c(leaving)
        if layer > 0:
            received = [swap_half(terms[0])]
            other_split = prepare(place, *after(other_split, grad_z))
            leaving = after(leaving, diagonal, other_split[0])
        else:
            received = [None, swap_half(terms[1])]
            later, go = step_of((later, after(go, grad_z)))
            leaving = after(leaving, later)
            go = lax.ppermute(go, ("h", "c"), DIAGONAL)
            later = (later, go)
        *first, g_high, g_low = weight_rows(0, place, (grad_z, leaving), own_split, width)
        turned = (g_high, g_low)
        come = [plane_swap(first[1], 0)]
        if layer == 0:
            received[0] = swap_half(after(terms[0], received[1]))
        second = weight_rows(1, place, turned, other_split, width)
        come.append(plane_swap(second[1], 0))
        stay = (first[0], second[0])
        kept = own_terms(own_columns, place, after(grad_z, second[0]), ups, weight, layer)
        if layer > 0:
            away = over_h(after(output[2], kept))
            output = [(a, 0) for a in (output[0], over_c(output[1]), away, diagonal)]
        ups = [(kept, None)] + [(r, None) for r in received]
        results[layer] = lax.dynamic_index_in_dim(
            sums.reshape(3, 4, width), clip, axis=1, keepdims=False
        )

    sums = jnp.stack(results)
    sums = [sums[:, 0], sums[:, 1], sums[:, 2]]
    aways = merge(kept, 1, received[1], apart=True)
    later = (later[0], over_c(after(later[1], aways[0])))
    come[0] = after(come[0], sums, later[1])
    far_near = over_c(lax.ppermute(aways[0], ("h", "c"), DIAGONAL))
    near_sum, far_sum, near_go, far_go = step_of(
        (in_hbm(stay[0]), come[0]), (in_hbm(stay[1]), come[1]), cut=2
    )
    near_go, far_go = over_second(near_go), over_second(far_go)
    (go,) = step_of((far_sum, after(far_go, far_near)), cut=0)
    (later,) = step_of(later, cut=0)
    later = after(later, go)
    go = over_h(go)
    later = plane_gather(later)
    (total,) = step_of((near_sum, near_go), cut=0)
    output = unpack(place, [(after(array, total), i) for array, i in output], frames, waited=True)
    close = merge(kept, 0, after(received[0], output))
    far = over_c(over_h(after(aways[1], go)))
    (share,) = step_of((total, after(go, close, *later[1:])), cut=0)
    gathered = plane_gather(share, far)
    grad_in = [(close, 0), (over_c(close[frames:]), 0), (far_near, 0), (far, 0)]
    grad_in = unpack(place, grad_in, frames)
    grad_weights = assemble(place, after(later, share), 1)
    grad_weights = assemble(place, after(gathered, grad_in), 0, grad_weights)
    return (output, grad_in, grad_weights, *sums, sums[1])


def gelu_slope(value):
    return (
        0.5 * (1.0 + jax.scipy.special.erf(value / ROOT_TWO))
        + value * jnp.exp(-0.5 * value * value) / ROOT_TWO_PI
    )


def recur_step(decay, state, inputs):
    drive_t, valid_t = inputs
    pre = drive_t + decay * state
    state = state + valid_t * (jax.nn.gelu(pre, approximate=False) - state)
    return (state, state)


def back_step(decay, carry, inputs):
    upstream_t, valid_t, pre_t = inputs
    total = upstream_t + carry
    grad_pre = total * valid_t * gelu_slope(pre_t)
    carry = total * (1.0 - valid_t) + grad_pre * decay
    return (carry, grad_pre)


def add_piece(weight, piece):
    return jnp.dot(weight, piece, precision=HIGH, preferred_element_type=jnp.float32)


def weight_columns(grad_pre_norm, piece):
    return jnp.einsum("jf,kf->jk", grad_pre_norm, piece, precision=HIGH)


def split_features(inputs, weights, gains, shifts, decays, biases, lengths, frame_mask, grad_out):
    width, slots = inputs.shape
    clips, frames_len = frame_mask.shape
    frames = jnp.arange(frames_len, dtype=jnp.int32)
    valid_grid = (
        (frames[None, :] < lengths[:, None]) & ((frame_mask == 1) | (frames[None, :] == 0))
    ).astype(jnp.float32)
    valid = valid_grid.reshape(-1)
    valid_row = valid[None, :]
    valid_time = jnp.broadcast_to(valid_grid.T[:, :, None], (frames_len, clips, width)).reshape(
        frames_len, clips * width
    )
    count_local = jnp.sum(valid)

    def to_time(array):
        return jnp.transpose(array.reshape(width, clips, frames_len), (2, 1, 0)).reshape(
            frames_len, clips * width
        )

    def from_time(array):
        return jnp.transpose(array.reshape(frames_len, clips, width), (2, 1, 0)).reshape(
            width, slots
        )

    layer_in = inputs
    saved = []
    for layer_no in range(LAYERS):
        weight = weights[layer_no]
        gathered = lax.all_gather(layer_in, "neuron", axis=0, tiled=True)
        pre_norm = add_piece(weight, gathered)
        first_sum, count = lax.psum((jnp.sum(valid_row * pre_norm, axis=1), count_local), "batch")
        mean = first_sum / count
        centered = pre_norm - mean[:, None]
        var = lax.psum(jnp.sum(valid_row * centered * centered, axis=1), "batch") / count
        inv_std = lax.rsqrt(var + EPS)
        zhat = (pre_norm - mean[:, None]) * inv_std[:, None]
        drive = gains[layer_no][:, None] * zhat + (shifts[layer_no] + biases[layer_no])[:, None]
        drive_time = to_time(drive)
        decay_wide = jnp.tile(decays[layer_no], clips)
        start_state = jnp.zeros((clips * width,), jnp.float32)
        _, states = lax.scan(
            partial(recur_step, decay_wide), start_state, (drive_time, valid_time), unroll=8
        )
        saved.append((gathered, zhat, inv_std, drive_time, states, count))
        layer_in = layer_in + valid_row * from_time(states)
    upstream = grad_out
    grad_parts = [None] * LAYERS
    for layer_no in range(LAYERS - 1, -1, -1):
        gathered, zhat, inv_std, drive_time, states, count = saved[layer_no]
        decay_wide = jnp.tile(decays[layer_no], clips)
        gain = gains[layer_no]
        previous = jnp.concatenate([jnp.zeros_like(states[:1]), states[:-1]], axis=0)
        pre_time = drive_time + decay_wide[None, :] * previous
        grad_state = to_time(valid_row * upstream)
        start_carry = jnp.zeros((clips * width,), jnp.float32)
        _, grad_pre_time = lax.scan(
            partial(back_step, decay_wide),
            start_carry,
            (grad_state, valid_time, pre_time),
            reverse=True,
            unroll=8,
        )
        decay_local = jnp.sum(
            jnp.sum(grad_pre_time * previous, axis=0).reshape(clips, width), axis=0
        )
        grad_pre = from_time(grad_pre_time)
        gain_local = jnp.sum(grad_pre * zhat, axis=1)
        shift_local = jnp.sum(grad_pre, axis=1)
        grad_gain, grad_shift, grad_decay = lax.psum(
            (gain_local, shift_local, decay_local), "batch"
        )
        grad_pre_norm = (gain * inv_std)[:, None] * (
            grad_pre - valid_row * (grad_shift[:, None] + zhat * grad_gain[:, None]) / count
        )
        weight_local = weight_columns(grad_pre_norm, gathered)
        input_terms = jnp.einsum("jk,jf->kf", weights[layer_no], grad_pre_norm, precision=HIGH)
        input_grad = lax.psum_scatter(input_terms, "neuron", scatter_dimension=0, tiled=True)
        grad_weight = lax.psum(weight_local, "batch")
        upstream = upstream + input_grad
        grad_parts[layer_no] = (grad_weight, grad_gain, grad_shift, grad_decay)
    grad_weights = jnp.stack([grad_parts[layer_no][0] for layer_no in range(LAYERS)])
    grad_gains = jnp.stack([grad_parts[layer_no][1] for layer_no in range(LAYERS)])
    grad_shifts = jnp.stack([grad_parts[layer_no][2] for layer_no in range(LAYERS)])
    grad_decays = jnp.stack([grad_parts[layer_no][3] for layer_no in range(LAYERS)])
    return (layer_in, upstream, grad_weights, grad_gains, grad_shifts, grad_decays, grad_shifts)


def solution(mesh):
    if (mesh.shape["batch"], mesh.shape["neuron"]) == (4, 8):
        cut = Mesh(mesh.devices.reshape(2, 2, 2, 2, 2), ("y", "x", "h", "l", "c"))
        batch, neuron, body = ("y", "x"), ("h", "l", "c"), half_features
    else:
        cut, batch, neuron, body = mesh, "batch", "neuron", split_features
    in_specs = (
        P(neuron, batch),
        P(None, neuron, None),
        P(None, neuron),
        P(None, neuron),
        P(None, neuron),
        P(None, neuron),
        P(batch),
        P(batch, None),
        P(neuron, batch),
    )
    out_specs = (
        P(neuron, batch),
        P(neuron, batch),
        P(None, neuron, None),
        P(None, neuron),
        P(None, neuron),
        P(None, neuron),
        P(None, neuron),
    )
    return jax.shard_map(
        body, mesh=cut, in_specs=in_specs, out_specs=out_specs, check_vma=False
    )
```

```python
from functools import partial
import math

import jax
import jax.numpy as jnp
from jax import lax
from jax.experimental import pallas as pl
from jax.experimental.pallas import tpu as pltpu
from jax.sharding import Mesh, PartitionSpec as P

LAYERS = 2
EPS = 1e-05
HIGH = lax.Precision.HIGHEST
ROOT_TWO = math.sqrt(2.0)
ROOT_TWO_PI = math.sqrt(2.0 * math.pi)
F32 = jnp.float32
BF16 = jnp.bfloat16
LANES = 128
VMEM_LIMIT = 24 * 1024 * 1024
SMEM_SPEC = pl.BlockSpec(memory_space=pltpu.SMEM)
VMEM_SPEC = pl.BlockSpec(memory_space=pltpu.VMEM)


FLIP2 = [(0, 1), (1, 0)]
DIAGONAL = [(0, 3), (1, 2), (2, 1), (3, 0)]


def swap_half(array):
    return lax.ppermute(array, "l", FLIP2)


def after(value, *others):
    return lax.optimization_barrier((value, others))[0]


def split(value):
    high = value.astype(BF16)
    return high, (value - high.astype(F32)).astype(BF16)


def dot(a, b, dims):
    return lax.dot_general(a, b, (dims, ((), ())), preferred_element_type=F32)


NT = ((1,), (1,))
NN = ((1,), (0,))


def in_hbm(array):
    return pltpu.with_memory_space_constraint(array, pltpu.HBM)


def call(body, out_shape, hbm_outs=(), **kwargs):
    if hbm_outs:
        out_shape = [
            pltpu.HBM(a.shape, a.dtype) if i in hbm_outs else a for i, a in enumerate(out_shape)
        ]
    return pl.pallas_call(
        body,
        out_shape=out_shape,
        compiler_params=pltpu.CompilerParams(vmem_limit_bytes=VMEM_LIMIT),
        **kwargs,
    )


def cost(flops, byte_count):
    return pl.CostEstimate(flops=int(flops) // 64, bytes_accessed=int(byte_count) // 64, transcendentals=0)


def pack_body(frames, place_ref, in_ref, near_ref, far_ref, turned):
    slots = in_ref.shape[1]
    for start in range(0, slots, LANES):
        turned[start : start + LANES, :] = in_ref[:, start : start + LANES].T
    for rel in range(4):
        first = pl.multiple_of(place_ref[rel] * frames, 8)
        out = (near_ref, far_ref)[rel // 2]
        out[(rel % 2) * frames : (rel % 2 + 1) * frames, :] = turned[pl.ds(first, frames), :]


def pack(place, array, frames, waits=False):
    width, slots = array.shape
    out = jax.ShapeDtypeStruct((2 * frames, width), F32)
    return call(
        partial(pack_body, frames),
        grid=(1,),
        out_shape=[out, out],
        in_specs=[SMEM_SPEC, pl.BlockSpec((width, slots), lambda i: (0, 0))],
        out_specs=[pl.BlockSpec(out.shape, lambda i: (0, 0))] * 2,
        scratch_shapes=[pltpu.VMEM((slots, width), F32)],
        hbm_outs=(0, 1) if waits else (),
        cost_estimate=cost(0, 8 * width * slots),
        name="pack",
    )(place, in_hbm(array))


def part_spec(part, frames):
    array, i = part
    if i is None:
        return pl.BlockSpec(array.shape, lambda *_: (0,) * array.ndim)
    return pl.BlockSpec((frames, array.shape[1]), lambda *_: (i, 0))


def arrays_of(parts):
    return [array for array, _ in parts]


def unpack_body(frames, place_ref, *refs):
    ins, out_ref, turned = refs[:4], refs[4], refs[5]
    slots = out_ref.shape[1]
    for rel in range(4):
        first = pl.multiple_of(place_ref[rel] * frames, 8)
        turned[pl.ds(first, frames), :] = ins[rel][...]
    for start in range(0, slots, LANES):
        out_ref[:, start : start + LANES] = turned[start : start + LANES, :].T


def unpack(place, parts, frames, waited=False):
    width = parts[0][0].shape[1]
    slots = 4 * frames
    return call(
        partial(unpack_body, frames),
        grid=(1,),
        out_shape=jax.ShapeDtypeStruct((width, slots), F32),
        in_specs=[SMEM_SPEC] + [part_spec(part, frames) for part in parts],
        out_specs=pl.BlockSpec((width, slots), lambda i: (0, 0)),
        scratch_shapes=[pltpu.VMEM((slots, width), F32)],
        cost_estimate=cost(0, 8 * width * slots),
        name="unpack",
    )(place, *[in_hbm(a) if waited else a for a in arrays_of(parts)])


def merge_body(kept_ref, come_ref, *outs):
    frames, columns = kept_ref.shape
    width = columns // 2
    for i in range(2):
        some = slice(i * width, (i + 1) * width)
        if len(outs) > 1:
            outs[i][...] = kept_ref[:, some] + come_ref[:, some]
            continue
        (out_ref,) = outs
        out_ref[i * frames : (i + 1) * frames, :] = kept_ref[:, some] + come_ref[:, some]


def merge(kept, half, come, apart=False):
    frames, columns = come.shape
    rows, n = (frames, 2) if apart else (2 * frames, 1)
    outs = call(
        merge_body,
        grid=(1,),
        out_shape=[jax.ShapeDtypeStruct((rows, columns // 2), F32)] * n,
        in_specs=[
            pl.BlockSpec((frames, columns), lambda i: (0, half)),
            pl.BlockSpec((frames, columns), lambda i: (0, 0)),
        ],
        out_specs=[pl.BlockSpec((rows, columns // 2), lambda i: (0, 0))] * n,
        cost_estimate=cost(0, 12 * frames * columns),
        name="merge",
    )(kept, come)
    return outs if apart else outs[0]


def project_body(n_parts, n_flat, spots, n_weights, first, with_acc, with_stats, with_params, cols_ref, place_ref, *refs):
    del cols_ref

    def take(n):
        nonlocal refs
        some, refs = refs[:n], refs[n:]
        return some

    parts, flat_parts, weights = take(n_parts), take(n_flat), take(n_weights)
    acc, valid, stats_in, params = take(with_acc), take(with_stats > 0), take(with_stats > 1), take(with_params)
    (out_ref,) = take(1)
    stats, flat = take(with_stats > 0), take(n_flat > 0)
    x_high, x_low, far_ref = refs
    step = pl.program_id(0)
    width = x_high.shape[2]

    @pl.when(step == 0)
    def _():
        for block, part in zip(spots, parts):
            for start in range(0, part.shape[1], width):
                high, low = split(part[:, start : start + width])
                x_high[block + start // width] = high
                x_low[block + start // width] = low
        column = 0
        for part in flat_parts:
            flat[0][:, column : column + part.shape[1]] = part[...]
            column += part.shape[1]
        if with_acc:
            out_ref[...] = acc[0][...]
        else:
            out_ref[...] = jnp.zeros_like(out_ref)

    stacked = jnp.concatenate([x_high[step], x_low[step], x_high[step]], axis=1)
    for block, weight in enumerate(weight_blocks(place_ref, weights, far_ref)):
        w_high, w_low = split(weight)
        columns = slice(block * width, (block + 1) * width)
        out_ref[:, columns] += dot(stacked, jnp.concatenate([w_high, w_high, w_low], axis=1), NT)

    if with_stats:
        (stats_ref,) = stats

        @pl.when(step == pl.num_programs(0) - 1)
        def _():
            if stats_in:
                stats_ref[...] = stats_in[0][...]
            own = jnp.sum(valid[0][...], axis=0, keepdims=True)
            per = width // LANES
            for row in range(out_ref.shape[1] // LANES):
                z = out_ref[:, row * LANES : (row + 1) * LANES]
                total = jnp.sum(valid[0][...] * z, axis=0, keepdims=True)
                centred = valid[0][...] * (z - total / own)
                squares = jnp.sum(centred * centred, axis=0, keepdims=True)
                at = place_ref[first + row // per] * per + row % per
                stats_ref[0, pl.ds(at, 1), :] = total
                stats_ref[1, pl.ds(at, 1), :] = squares
                stats_ref[2, pl.ds(at, 1), :] = own
            if with_params:
                rest = params[0].shape[0] - 8
                stats_ref[3] = params[0][:8, :]
                stats_ref[4] = jnp.zeros_like(stats_ref[4])
                stats_ref[4, :rest, :] = params[0][8:, :]


def weight_specs(weights, layer, pairs=2):
    specs = []
    for weight in weights:
        if weight.ndim == 3:
            shape = (1, weight.shape[1], pairs * weight.shape[1])
            specs.append(pl.BlockSpec(shape, lambda s, cols, *_: (layer, 0, cols[s])))
        else:
            shape = (weight.shape[0], pairs * 4 * weight.shape[0])
            specs.append(pl.BlockSpec(shape, lambda s, cols, *_: (0, cols[s])))
    return specs


def far_scratch(width, pairs=2):
    return pltpu.VMEM((2, width, pairs * width), F32)


def weight_blocks(place_ref, refs, far_ref):
    near = [ref[0] for ref in refs if len(ref.shape) == 3]
    pieces = [ref for ref in refs if len(ref.shape) == 2]
    far = []
    for i in range(len(pieces) // 4):
        for rel, piece in enumerate(pieces[4 * i : 4 * i + 4]):
            rows = piece.shape[0]
            row = 2 * (place_ref[4] ^ (rel // 2)) + (place_ref[5] ^ (rel % 2))
            far_ref[i, pl.ds(pl.multiple_of(row * rows, rows), rows), :] = piece[...]
        far.append(far_ref[i])
    return near + far


def project(
    place, frames, parts, blocks, weights, layer, acc=None, valid=None, stats=None, params=None, flat=()
):
    near = weights[0].ndim == 3
    units = sum(1 if w.ndim == 3 else 0.25 for w in weights)
    width = weights[0].shape[1] if near else 4 * weights[0].shape[0]
    n = blocks.shape[0]
    spots, block = [], 0
    for array, _ in parts:
        spots.append(block)
        block += array.shape[1] // width
    full = pl.BlockSpec(memory_space=pltpu.VMEM)
    in_specs = [part_spec(part, frames) for part in (*parts, *flat)]
    in_specs += weight_specs(weights, layer, 1)
    operands = arrays_of(parts) + arrays_of(flat) + [in_hbm(w) for w in weights]
    array = jax.ShapeDtypeStruct((frames, int(units) * width), F32)
    array_spec = pl.BlockSpec(array.shape, lambda s, cols, place: (0, 0))
    out_shape, out_specs = [array], [array_spec]
    if acc is not None:
        in_specs.append(array_spec)
        operands.append(in_hbm(acc))
    if valid is not None:
        in_specs.append(full)
        operands.append(valid)
        shape = (3 if params is None else 5, 4 * width // LANES, LANES)
        out_shape.append(jax.ShapeDtypeStruct(shape, F32))
        out_specs.append(pl.BlockSpec(shape, lambda s, cols, place: (0, 0, 0)))
    for extra in (stats, params):
        if extra is not None:
            in_specs.append(full)
            operands.append(extra)
    if flat:
        out_shape.append(jax.ShapeDtypeStruct((frames, 4 * width), F32))
        out_specs.append(pl.BlockSpec((frames, 4 * width), lambda s, cols, place: (0, 0)))
    return call(
        partial(
            project_body,
            len(parts),
            len(flat),
            spots,
            len(weights),
            0 if near else 2,
            acc is not None,
            (valid is not None) + (stats is not None),
            params is not None,
        ),
        grid_spec=pltpu.PrefetchScalarGridSpec(
            num_scalar_prefetch=2,
            grid=(n,),
            in_specs=in_specs,
            out_specs=out_specs,
            scratch_shapes=[pltpu.VMEM((n, frames, width), BF16)] * 2 + [far_scratch(width, 1)],
        ),
        out_shape=out_shape,
        hbm_outs=(0, len(out_shape) - 1) if flat else (0,),
        cost_estimate=cost(6 * frames * n * width * units * width, 4 * n * width * units * width),
        name="project",
    )(blocks, place, *operands)


def to_relative(place_ref, spread, rows_ref, value, slot):
    per = value.shape[0] // 4
    spread[...] = value
    for rel in range(4):
        first = place_ref[rel] * per
        for row in range(per):
            rows_ref[slot, rel * per + row : rel * per + row + 1, :] = spread[
                pl.ds(first + row, 1), :
            ]


def tree(values):
    while len(values) > 1:
        values = [a + b for a, b in zip(values[::2], values[1::2])]
    return values[0]


def gathered(ref, slot):
    return [ref[i] for i in range(slot, ref.shape[0], ref.shape[0] // 16)]


def norm_terms(stats_ref):
    each = [gathered(stats_ref, slot) for slot in range(3)]
    totals, squares, owns = each
    count = tree(owns)
    mean = tree(totals) / count
    away = [total / own - mean for total, own in zip(totals, owns)]
    spread = tree([s + n * a * a for s, n, a in zip(squares, owns, away)])
    return count, mean, lax.rsqrt(spread / count + EPS)


CHUNKS = 4


def columns_of(refs, row):
    for ref in refs:
        if row * LANES < ref.shape[1]:
            return ref[:, row * LANES : (row + 1) * LANES]
        row -= ref.shape[1] // LANES


def recur_body(n_z, last, layer, spread_params, place_ref, gate_ref, *refs):
    z_refs, refs = refs[:n_z], refs[n_z:]
    (stats_ref, params_ref, valid_ref, x_ref), refs = refs[:4], refs[4:]
    outs, refs = refs[: 1 + 3 * last], refs[1 + 3 * last :]
    if spread_params:
        state_ref, slope_ref, params_out, rows, spread, held, drive_s, state_s, slope_s = refs
    else:
        state_ref, slope_ref, rows, spread, held, drive_s, state_s, slope_s = refs
    frames, features = x_ref.shape
    blocks = features // LANES
    per = blocks // 4
    chunk = pl.program_id(0)

    @pl.when(chunk == 0)
    def _():
        if spread_params:
            for rel in range(4):
                first = place_ref[rel] * (stats_ref.shape[0] // 16) + 3
                for row in range(LAYERS * 3 * per):
                    at = rel * per + row % per
                    params_out[row // per, at : at + 1, :] = stats_ref[
                        first + row // 8, row % 8 : row % 8 + 1, :
                    ]
            params = [params_out[3 * layer + i] for i in range(3)]
        else:
            params = [params_ref[3 * layer + i] for i in range(3)]
        _, mean, inv_std = norm_terms(stats_ref)
        to_relative(place_ref, spread, rows, mean, 0)
        to_relative(place_ref, spread, rows, inv_std, 1)
        rows[1] = rows[1] * params[0]
        rows[2] = params[1]
        rows[3] = params[2]
        held[...] = jnp.zeros_like(held)

    for row in range(blocks):
        drive_s[row * frames : (row + 1) * frames, :] = (
            columns_of(z_refs, row) - rows[0, row : row + 1, :]
        ) * rows[1, row : row + 1, :] + rows[2, row : row + 1, :]
    decay = rows[3]

    def step(t, state):
        at = pl.ds(t, blocks, stride=frames)
        pre = drive_s[at, :] + decay * state
        half = 0.5 + 0.5 * lax.erf(pre * (1.0 / ROOT_TWO))
        gate = gate_ref[chunk * frames + t] > 0.0
        slope = half + pre * jnp.exp(-0.5 * pre * pre) * (1.0 / ROOT_TWO_PI)
        state = jnp.where(gate, pre * half, state)
        state_s[at, :] = state
        slope_s[at, :] = jnp.where(gate, slope, 0.0)
        return state

    held[...] = lax.fori_loop(0, frames, step, held[...], unroll=8)
    valid = valid_ref[...]
    for row in range(blocks):
        lanes = slice(row * LANES, (row + 1) * LANES)
        state = state_s[row * frames : (row + 1) * frames, :]
        state_ref[:, lanes] = state
        slope_ref[:, lanes] = slope_s[row * frames : (row + 1) * frames, :]
        value = x_ref[:, lanes] + valid * state
        out, at = (outs[row // per], row % per) if last else (outs[0], row)
        out[:, at * LANES : (at + 1) * LANES] = value


def recur(layer, place, gate, z, stats, params, valid, x, last):
    frames, features = x.shape
    blocks = features // LANES
    some = frames // CHUNKS
    whole = lambda array: pl.BlockSpec(array.shape, lambda i: (0,) * array.ndim)
    by_chunk = lambda array: pl.BlockSpec((some, array.shape[1]), lambda i: (i, 0))
    full = jax.ShapeDtypeStruct((frames, features), F32)
    piece = jax.ShapeDtypeStruct((frames, features // 4), F32)
    out_shape = [piece] * 4 if last else [full]
    out_shape += [full, full]
    out_specs = [by_chunk(a) for a in out_shape]
    spread_params = params is None
    if spread_params:
        out_shape.append(jax.ShapeDtypeStruct((3 * LAYERS, blocks, LANES), F32))
        out_specs.append(whole(out_shape[-1]))
        params = valid
    return call(
        partial(recur_body, len(z), last, layer, spread_params),
        grid=(CHUNKS,),
        in_specs=[SMEM_SPEC, SMEM_SPEC]
        + [by_chunk(a) for a in z]
        + [whole(a) for a in (stats, params)]
        + [by_chunk(a) for a in (valid, x)],
        out_specs=out_specs,
        out_shape=out_shape,
        hbm_outs=tuple(range(len(out_shape) - spread_params)) if last else (1, 2),
        scratch_shapes=[
            pltpu.VMEM((4, blocks, LANES), F32),
            pltpu.VMEM((blocks, LANES), F32),
            pltpu.VMEM((blocks, LANES), F32),
        ]
        + [pltpu.VMEM((blocks * some, LANES), F32)] * 3,
        cost_estimate=cost(100 * frames * features, 20 * frames * features),
        name="recur",
    )(place, gate, *[in_hbm(a) for a in z], stats, params, valid, in_hbm(x))


def back_body(n_z, n_ups, spots, layer, place_ref, gate_ref, *refs):
    z_refs, refs = refs[:n_z], refs[n_z:]
    (stats_ref, params_ref), refs = refs[:2], refs[2:]
    ups, (state_ref, slope_ref), refs = refs[:n_ups], refs[n_ups : n_ups + 2], refs[n_ups + 2 :]
    grad_ref, sums_ref, rows, spread, held, up_s, state_s, slope_s = refs
    frames, features = state_ref.shape
    blocks = features // LANES
    per = blocks // 4
    tall = frames + 8
    step_no = pl.program_id(0)
    chunk = pl.num_programs(0) - 1 - step_no

    @pl.when(step_no == 0)
    def _():
        _, mean, inv_std = norm_terms(stats_ref)
        to_relative(place_ref, spread, rows, mean, 0)
        to_relative(place_ref, spread, rows, inv_std, 1)
        held[...] = jnp.zeros_like(held)

    for row in range(blocks):
        lanes = slice(row * LANES, (row + 1) * LANES)
        base = row * frames
        up = None
        for (_, column), part in zip(spots, ups):
            if column <= row * LANES < column + part.shape[1]:
                value = part[:, row * LANES - column : (row + 1) * LANES - column]
                up = value if up is None else up + value
        up_s[base : base + frames, :] = up
        state_s[row * tall : row * tall + 8, :] = jnp.zeros((8, LANES), F32)
        state_s[row * tall + 8 : (row + 1) * tall, :] = state_ref[:, lanes]
        slope_s[base : base + frames, :] = slope_ref[:, lanes]
    decay = params_ref[3 * layer + 2]

    def step(i, carry):
        t = frames - 1 - i
        at = pl.ds(t, blocks, stride=frames)
        slope = slope_s[at, :]
        gate = gate_ref[chunk * frames + t]
        total = gate * up_s[at, :] + carry
        up_s[at, :] = total * slope
        return total * (slope * decay + (1.0 - gate))

    held[0] = lax.fori_loop(0, frames, step, held[0], unroll=8)
    held[4] += held[1] * state_s[pl.ds(tall - 1, blocks, stride=tall), :]
    held[1] = up_s[pl.ds(0, blocks, stride=frames), :]
    for row in range(blocks):
        lanes = slice(row * LANES, (row + 1) * LANES)
        grad = up_s[row * frames : (row + 1) * frames, :]
        grad_ref[:, lanes] = grad
        zhat = (columns_of(z_refs, row) - rows[0, row : row + 1, :]) * rows[1, row : row + 1, :]
        before = state_s[row * tall + 7 : row * tall + 7 + frames, :]
        for slot, value in enumerate((grad * zhat, grad, grad * before)):
            held[2 + slot, row : row + 1, :] += jnp.sum(value, axis=0, keepdims=True)

    @pl.when(chunk == 0)
    def _():
        for row in range(blocks):
            at = place_ref[row // per] * per + row % per
            for slot in range(3):
                sums_ref[slot, pl.ds(at, 1), :] = held[2 + slot, row : row + 1, :]


def spots_of_sum(parts, width):
    spots, column = [], 0
    for array, _ in parts:
        spots.append((0, column % (4 * width)))
        column += array.shape[1]
    return spots


def back(layer, place, gate, z, stats, params, ups, states, slopes):
    frames, features = states.shape
    width = features // 4
    blocks = features // LANES
    some = frames // CHUNKS
    whole = lambda array: pl.BlockSpec(array.shape, lambda i: (0,) * array.ndim)

    def by_chunk(array, first=0):
        return pl.BlockSpec(
            (some, array.shape[1]), lambda i: ((first or 0) * CHUNKS + CHUNKS - 1 - i, 0)
        )

    out_shape = [
        jax.ShapeDtypeStruct((frames, features), F32),
        jax.ShapeDtypeStruct((3, blocks, LANES), F32),
    ]
    return call(
        partial(back_body, len(z), len(ups), spots_of_sum(ups, width), layer),
        grid=(CHUNKS,),
        in_specs=[SMEM_SPEC] * 2
        + [by_chunk(a) for a in z]
        + [whole(a) for a in (stats, params)]
        + [by_chunk(*up) for up in ups]
        + [by_chunk(a) for a in (states, slopes)],
        out_specs=[by_chunk(out_shape[0]), whole(out_shape[1])],
        out_shape=out_shape,
        scratch_shapes=[
            pltpu.VMEM((2, blocks, LANES), F32),
            pltpu.VMEM((blocks, LANES), F32),
            pltpu.VMEM((5, blocks, LANES), F32),
            pltpu.VMEM((blocks * some, LANES), F32),
            pltpu.VMEM((blocks * (some + 8), LANES), F32),
            pltpu.VMEM((blocks * some, LANES), F32),
        ],
        cost_estimate=cost(30 * frames * features, 20 * frames * features),
        name="back",
    )(
        place,
        gate,
        *[in_hbm(a) for a in z],
        stats,
        params,
        *arrays_of(ups),
        in_hbm(states),
        in_hbm(slopes),
    )


def input_terms(high_s, low_s, weights):
    left, right = [], []
    for block, weight in enumerate(weights):
        w_high, w_low = split(weight)
        left += [high_s[block], low_s[block], high_s[block]]
        right += [w_high, w_high, w_low]
    return dot(jnp.concatenate(left, axis=1), jnp.concatenate(right, axis=0), NN)


def norm_back_body(n_z, split_terms, layer, cols_ref, place_ref, grad_ref, *refs):
    del cols_ref
    z_refs, refs = refs[:n_z], refs[n_z:]
    params_ref, valid_ref, stats_ref, sums_ref, *refs = refs
    weights, refs = refs[:10], refs[10:]
    if split_terms:
        out_ref, leave_ref, near_term_ref, far_term_ref, sums_out_ref, *refs = refs
        term_refs, starts = (far_term_ref, near_term_ref), (0, 0)
    else:
        out_ref, leave_ref, term_ref, sums_out_ref, *refs = refs
        term_refs, starts = (term_ref, term_ref), (2 * grad_ref.shape[1] // 4, 0)
    rows, spread, high_s, low_s, far_ref = refs
    blocks = grad_ref.shape[1] // LANES
    width = high_s.shape[2]
    per = width // LANES

    @pl.when(pl.program_id(0) == 0)
    def _():
        count, mean, inv_std = norm_terms(stats_ref)
        to_relative(place_ref, spread, rows, mean, 0)
        to_relative(place_ref, spread, rows, inv_std, 1)
        rows[2] = rows[1] * params_ref[3 * layer]
        sums = [tree(gathered(sums_ref, slot)) for slot in range(3)]
        for slot in range(3):
            sums_out_ref[slot] = sums[slot]
        to_relative(place_ref, spread, rows, sums[0] / count, 3)
        to_relative(place_ref, spread, rows, sums[1] / count, 4)
        valid = valid_ref[...]
        for row in range(blocks):
            lanes = slice(row * LANES, (row + 1) * LANES)
            one = lambda slot: rows[slot, row : row + 1, :]
            zhat = (columns_of(z_refs, row) - one(0)) * one(1)
            value = one(2) * (grad_ref[:, lanes] - valid * (one(4) + zhat * one(3)))
            out_ref[:, lanes] = value
            if (row // per) % 2:
                at = (row // per // 2) * width + (row % per) * LANES
                leave_ref[:, at : at + LANES] = value
            high, low = split(value)
            inner = slice((row % per) * LANES, (row % per + 1) * LANES)
            high_s[row // per, :, inner] = high
            low_s[row // per, :, inner] = low

    value = input_terms(high_s, low_s, weight_blocks(place_ref, weights, far_ref))
    for step, (term_ref, first) in enumerate(zip(term_refs, starts)):

        @pl.when(pl.program_id(0) == step)
        def _():
            for pair in range(2):
                at = pl.multiple_of(((place_ref[0] & 1) ^ pair) * width, width)
                term_ref[:, pl.ds(first + at, width)] = value[
                    :, pair * width : (pair + 1) * width
                ]


def norm_back(columns, place, grad, z, params, valid, stats, sums, weights, layer, split_terms):
    frames, features = grad.shape
    width = features // 4
    blocks = features // LANES
    whole = lambda array: pl.BlockSpec(array.shape, lambda s, cols, place: (0,) * array.ndim)
    operands = [grad, *[in_hbm(a) for a in z], params, valid, stats, sums]
    full = jax.ShapeDtypeStruct((frames, features), F32)
    half = jax.ShapeDtypeStruct((frames, 2 * width), F32)
    terms = [half, half] if split_terms else [full]
    out_shape = [full, half, *terms, jax.ShapeDtypeStruct((3, blocks, LANES), F32)]
    return call(
        partial(norm_back_body, len(z), split_terms, layer),
        grid_spec=pltpu.PrefetchScalarGridSpec(
            num_scalar_prefetch=2,
            grid=(2,),
            in_specs=[whole(a) for a in operands] + weight_specs(weights, layer),
            out_specs=[whole(a) for a in out_shape],
            scratch_shapes=[
                pltpu.VMEM((5, blocks, LANES), F32),
                pltpu.VMEM((blocks, LANES), F32),
                pltpu.VMEM((4, frames, width), BF16),
                pltpu.VMEM((4, frames, width), BF16),
                far_scratch(width),
            ],
        ),
        out_shape=out_shape,
        hbm_outs=(0,),
        cost_estimate=cost(6 * frames * features * features, 4 * features * features),
        name="norm_back",
    )(columns, place, *operands, *[in_hbm(w) for w in weights])


def own_terms_body(n_ups, spots, cols_ref, place_ref, grad_ref, *refs):
    del cols_ref
    ups, refs = refs[:n_ups], refs[n_ups:]
    weights, refs = refs[:10], refs[10:]
    out_ref, high_s, low_s, far_ref = refs
    width = high_s.shape[2]
    step = pl.program_id(0)

    @pl.when(step == 0)
    def _():
        for block in range(4):
            high, low = split(grad_ref[:, block * width : (block + 1) * width])
            high_s[block] = high
            low_s[block] = low

    value = input_terms(high_s, low_s, weight_blocks(place_ref, weights, far_ref))
    for pair in range(2):
        at = pl.multiple_of(((place_ref[0] & 1) ^ pair) * width, width)
        out_ref[:, pl.ds(at, width)] = value[:, pair * width : (pair + 1) * width]
    for half in range(2):

        @pl.when(step == half)
        def _():
            first = 2 * half * width
            for (_, column), up in zip(spots, ups):
                low = max(column, first)
                high = min(column + up.shape[1], first + 2 * width)
                if low < high:
                    out_ref[:, low - first : high - first] += up[:, low - column : high - column]


def own_terms(columns, place, grad, ups, weights, layer):
    frames, features = grad.shape
    width = features // 4
    whole = lambda array: pl.BlockSpec(array.shape, lambda s, cols, place: (0,) * array.ndim)
    step_block = pl.BlockSpec((frames, 2 * width), lambda s, cols, place: (0, s))
    return call(
        partial(own_terms_body, len(ups), spots_of_sum(ups, width)),
        grid_spec=pltpu.PrefetchScalarGridSpec(
            num_scalar_prefetch=2,
            grid=(2,),
            in_specs=[whole(grad)]
            + [part_spec(up, frames) for up in ups]
            + weight_specs(weights, layer),
            out_specs=step_block,
            scratch_shapes=[pltpu.VMEM((4, frames, width), BF16)] * 2 + [far_scratch(width)],
        ),
        out_shape=jax.ShapeDtypeStruct((frames, features), F32),
        cost_estimate=cost(6 * frames * features * features, 4 * features * features),
        name="own_terms",
    )(columns, place, in_hbm(grad), *arrays_of(ups), *[in_hbm(w) for w in weights])


def prepare_body(lists_ref, place_ref, own_ref, near_ref, high_ref, low_ref):
    del lists_ref
    padded = high_ref.shape[0] // 2
    width = high_ref.shape[1] // 2
    for clip, part in enumerate((own_ref, near_ref)):
        rows = part.shape[0]
        for dc in range(2):
            at = pl.multiple_of((place_ref[6] ^ clip ^ dc) * width, width)
            high, low = split(part[:, dc * width : (dc + 1) * width])
            high_ref[clip * padded : clip * padded + rows, pl.ds(at, width)] = high
            low_ref[clip * padded : clip * padded + rows, pl.ds(at, width)] = low
        zeros = jnp.zeros((padded - rows, 2 * width), BF16)
        high_ref[clip * padded + rows : (clip + 1) * padded, :] = zeros
        low_ref[clip * padded + rows : (clip + 1) * padded, :] = zeros


def prepare(place, own, near):
    frames, features = own.shape
    width = features // 4
    padded = -(-frames // LANES) * LANES
    in_spec = pl.BlockSpec((frames, 2 * width), lambda s, *_: (0, s))
    out = jax.ShapeDtypeStruct((2 * padded, features), BF16)
    out_spec = pl.BlockSpec((2 * padded, 2 * width), lambda s, order, place: (0, order[s]))
    order = jnp.stack([place[0] >> 1, 1 - (place[0] >> 1)])
    return call(
        prepare_body,
        grid_spec=pltpu.PrefetchScalarGridSpec(
            num_scalar_prefetch=2,
            grid=(2,),
            in_specs=[in_spec, in_spec],
            out_specs=[out_spec, out_spec],
        ),
        out_shape=[out, out],
        hbm_outs=(0, 1),
        cost_estimate=cost(0, 16 * frames * features),
        name="prepare",
    )(order, place, in_hbm(own), in_hbm(near))


def product(g_high, g_low, x_high, x_low):
    return dot(g_high, x_high, NN) + (dot(g_high, x_low, NN) + dot(g_low, x_high, NN))


def weight_body(turn, place_ref, *refs):
    if turn:
        grad_ref, near_ref, x_high, x_low, kept, sent, g_high, g_low, t_high, t_low = refs

        @pl.when(pl.program_id(0) == 0)
        def _():
            frames, features = grad_ref.shape
            width = features // 4
            rows = width // 4
            padded = t_high.shape[1] // 2
            t_high[...] = jnp.zeros_like(t_high)
            t_low[...] = jnp.zeros_like(t_low)
            for clip in range(2):
                for dh in range(2):
                    if clip == 0:
                        part = grad_ref[:, 2 * dh * width : (2 * dh + 1) * width]
                    else:
                        part = near_ref[:, dh * width : (dh + 1) * width]
                    high, low = split(part.T)
                    at = (
                        slice(dh * width, (dh + 1) * width),
                        slice(clip * padded, clip * padded + frames),
                    )
                    t_high[at] = high
                    t_low[at] = low
            for group in range(8):
                first, second, dh = group // 4, group // 2 % 2, group % 2
                core = place_ref[6]
                y = place_ref[4] ^ (first * core + second * (1 - core))
                x = place_ref[5] ^ (first * (1 - core) + second * core)
                at = pl.multiple_of(dh * width + (2 * y + x) * rows, rows)
                g_high[group * rows : (group + 1) * rows, :] = t_high[pl.ds(at, rows), :]
                g_low[group * rows : (group + 1) * rows, :] = t_low[pl.ds(at, rows), :]

    else:
        g_high, g_low, x_high, x_low, kept, sent = refs
    half = g_high.shape[0] // 2
    value = product(g_high[...], g_low[...], x_high[...], x_low[...])
    kept[...] = value[:half].reshape(kept.shape)
    sent[...] = value[half:].reshape(sent.shape)


def weight_rows(side, place, grads, x_split, width):
    turn = side == 0
    whole = lambda array: pl.BlockSpec(array.shape, lambda s, place: (0,) * array.ndim)
    x_spec = pl.BlockSpec((x_split[0].shape[0], width), lambda s, place: (0, s))
    shape = (2, 2, width // 4, 4 * width)
    out_shape = [jax.ShapeDtypeStruct(shape, F32)] * 2
    out_specs = [pl.BlockSpec(shape[:3] + (width,), lambda s, place: (0, 0, 0, s))] * 2
    scratch = []
    if turn:
        turned = (2 * width, x_split[0].shape[0])
        out_shape += [jax.ShapeDtypeStruct(turned, BF16)] * 2
        out_specs += [whole(out_shape[-1])] * 2
        scratch = [pltpu.VMEM(turned, BF16)] * 2
    return call(
        partial(weight_body, turn),
        grid_spec=pltpu.PrefetchScalarGridSpec(
            num_scalar_prefetch=1,
            grid=(4,),
            in_specs=[whole(a) for a in grads] + [x_spec] * 2,
            out_specs=out_specs,
            scratch_shapes=scratch,
        ),
        out_shape=out_shape,
        hbm_outs=(0,),
        cost_estimate=cost(12 * x_split[0].shape[0] * width * 4 * width, 4 * 8 * width * width),
        name="weight_rows",
    )(place, *([in_hbm(grads[0]), grads[1]] if turn else grads), *[in_hbm(x) for x in x_split])


def step_body(n, widths, cut, *refs):
    ins, outs = refs[: 2 * n], refs[2 * n :]
    starts = [sum(widths[:i]) for i in range(len(widths))]
    column = 0
    for i in range(n):
        total = ins[2 * i][...] + ins[2 * i + 1][...]
        end = column + total.shape[-1]
        for j, (start, columns) in enumerate(zip(starts, widths)):
            low, high = max(start, column), min(start + columns, end)
            if low < high:
                to = (Ellipsis, slice(low - start, high - start))
                piece = total[..., low - column : high - column]
                pieces = [piece]
                for _ in range(cut):
                    pieces = [half[k] for half in pieces for k in range(2)]
                for k, some in enumerate(pieces):
                    outs[len(pieces) * j + k][to] = some
        column = end


def step_of(*pairs, cut=1, widths=None):
    shape = list(pairs[0][0].shape)
    widths = widths or [sum(pair[0].shape[-1] for pair in pairs)]
    outs = []
    for columns in widths:
        shape[-1] = columns
        outs += [jax.ShapeDtypeStruct(tuple(shape[cut:]), F32)] * 2**cut
    whole = lambda array: pl.BlockSpec(array.shape, lambda i: (0,) * array.ndim)
    operands = [array for pair in pairs for array in pair]
    return call(
        partial(step_body, len(pairs), widths, cut),
        grid=(1,),
        in_specs=[whole(a) for a in operands],
        out_specs=[whole(a) for a in outs],
        out_shape=outs,
        cost_estimate=cost(0, 4 * sum(a.size for a in operands)),
        name="reduction_step",
    )(*operands)


def plane_swap(array, step):
    pairs = []
    for i in range(8):
        over_x = (i % 2 == 0) == (step == 0)
        pairs.append((i, i ^ 2 if over_x else i ^ 4))
    return lax.ppermute(array, ("y", "x", "c"), pairs)


def plane_gather(share):
    first = plane_swap(share, 0)
    second = plane_swap(share, 1)
    return [share, second, first, plane_swap(after(first, second), 1)]


def assemble_body(place_ref, *refs):
    out_ref = refs[-1]
    core = place_ref[6]
    rows, columns = refs[0].shape
    quarter = columns // 4
    for i in range(4):
        first, second = i // 2, i % 2
        y = place_ref[4] ^ (first * core + second * (1 - core))
        x = place_ref[5] ^ (first * (1 - core) + second * core)
        at = pl.multiple_of((2 * y + x) * rows, rows)
        for side in range(2):
            for h in range(2):
                to = pl.multiple_of((2 * h + (place_ref[7] ^ side)) * quarter, quarter)
                some = slice((2 * side + h) * quarter, (2 * side + h + 1) * quarter)
                out_ref[0, pl.ds(at, rows), pl.ds(to, quarter)] = refs[i][:, some]


def assemble(place, pieces, layer, onto=None):
    rows, columns = 4 * pieces[0].shape[0], pieces[0].shape[1]
    aliases, extra, extra_specs = {}, [], []
    if onto is not None:
        aliases, extra = {1 + len(pieces): 0}, [onto]
        extra_specs = [pl.BlockSpec(memory_space=pl.ANY)]
    (out,) = call(
        assemble_body,
        grid=(1,),
        out_shape=[jax.ShapeDtypeStruct((LAYERS, rows, columns), F32)],
        hbm_outs=(0,),
        in_specs=[SMEM_SPEC]
        + [pl.BlockSpec(p.shape, lambda i: (0, 0)) for p in pieces]
        + extra_specs,
        out_specs=[pl.BlockSpec((1, rows, columns), lambda i: (layer, 0, 0))],
        input_output_aliases=aliases,
        cost_estimate=cost(0, 8 * rows * columns),
        name="assemble",
    )(place, *[p if extra else in_hbm(p) for p in pieces], *extra)
    return out


def half_features(inputs, weights, gains, shifts, decays, biases, lengths, frame_mask, grad_out):
    width, slots = inputs.shape
    clips, frames = frame_mask.shape
    depth = weights.shape[2]
    blocks = 4 * width // LANES
    y, x, h, l, c = (lax.axis_index(name) for name in ("y", "x", "h", "l", "c"))
    b = 2 * y + x
    numbers = [2 * (h ^ (rel // 2)) + (c ^ (rel % 2)) for rel in range(4)] + [y, x, c, l]
    place = jnp.stack(numbers).astype(jnp.int32)
    own_blocks, other_blocks = (
        jnp.stack(
            [2 * (2 * (h ^ (rel // 2)) + half) + (c ^ (rel % 2)) for rel in range(4)]
        ).astype(jnp.int32)
        for half in (l, 1 - l)
    )
    own_columns = jnp.stack([2 * h + l, 2 * (1 - h) + l]).astype(jnp.int32)
    other_columns = jnp.stack([2 * (1 - h) + 1 - l, 2 * h + 1 - l]).astype(jnp.int32)
    rows = width // 4

    clip = 2 * h + c
    seen = lax.dynamic_index_in_dim(frame_mask, clip, 0, keepdims=False)
    length = lax.dynamic_index_in_dim(lengths, clip, 0, keepdims=False)
    moments = jnp.arange(frames, dtype=jnp.int32)
    gate = ((moments < length) & ((seen == 1) | (moments == 0))).astype(F32)
    valid = jnp.broadcast_to(gate[:, None], (frames, LANES))

    def far_share(layer):
        return lax.dynamic_slice(weights, (layer, b * rows, 0), (1, rows, depth))[0]

    def over_h(array):
        return lax.ppermute(array, "h", FLIP2)

    def over_c(array):
        return lax.ppermute(array, "c", FLIP2)

    def over_second(array):
        return plane_swap(array, 1)

    def four_of(near_rows, far_rows):
        return [
            (near_rows, 0),
            (over_c(near_rows), 1),
            (far_rows, 0),
            (over_c(far_rows), 1),
        ]

    def four_of_plane(share):
        both = lax.ppermute(share, ("y", "x"), DIAGONAL)
        return [share, lax.ppermute(share, "x", FLIP2), lax.ppermute(share, "y", FLIP2), both]

    near = over_c(weights)
    share = far_share(0)
    close, away = pack(place, after(inputs, share), frames)
    share = over_h(share)
    away = over_h(away)
    other_close = swap_half(close)
    up_close, up_away = pack(place, after(grad_out, close), frames, waits=True)
    share = after(share, up_close, valid, near, other_close)
    pieces = four_of_plane(share)
    away = after(away, pieces[1:])
    half_weights = [[weights, near, *pieces, *map(over_c, after(pieces, away))]]
    own = four_of(after(close, away), away)
    other_away = swap_half(away)
    others = [(other_close, 0), (over_c(other_close), 1)]
    params = jnp.stack([gains, shifts + biases, decays], axis=1)
    own_params = params.reshape(LAYERS * 3 * width // LANES, LANES)
    params = None

    def gather(array, axes):
        return lax.all_gather(array, axes, tiled=True)

    weight = half_weights[0]
    early = jnp.concatenate([own_blocks, other_blocks[:2]])
    z, own_flat = project(place, frames, own + others, early, weight, 0, flat=own)
    others += [(other_away, 0), (over_c(after(other_away, z)), 1)]
    z, stats, other_flat = project(
        place,
        frames,
        others[2:],
        other_blocks[2:],
        weight,
        0,
        z,
        valid,
        params=own_params,
        flat=others,
    )
    z = [z]
    stats = gather(stats, ("h", "c"))
    share = over_c(lax.ppermute(after(far_share(1), stats), ("h", "c"), DIAGONAL))
    stats = gather(stats, ("y", "x"))
    x, states, slopes, params = recur(0, place, gate, z, stats, None, valid, own_flat, False)
    own_near, other_near = over_c(after(own_flat, z[0])), over_c(after(other_flat, z[0]))
    x_near = over_c(x)
    own_split = prepare(place, after(own_flat, x_near), own_near)
    other_split = prepare(place, after(other_flat, x_near), other_near)
    saved = [(own_split, other_split, z, stats, states, slopes)]

    pieces = four_of_plane(after(share, slopes, own_near, other_near))
    near = [weights, near]
    other = swap_half(x)
    x_own = after(x, own_split[0], other_split[0])
    z, *_ = project(place, frames, [(x_own, None)], own_blocks, near, 1)
    own_split = prepare(place, after(x, z), x_near)
    far = [*pieces, *map(over_c, after(pieces, own_split[0]))]
    up_away = over_h(after(up_away, other, own_split[0]))
    half_weights.append(near + far)
    z, stats = project(place, frames, [(other, None)], other_blocks, near, 1, z, valid)
    both = jnp.concatenate([own_blocks, other_blocks])
    z_far, stats = project(
        place,
        frames,
        [(x, None), (other, None)],
        both,
        far,
        1,
        None,
        valid,
        stats,
    )
    z = [z, z_far]
    stats = gather(gather(stats, ("y", "x")), ("h", "c"))
    upstream = four_of(up_close, after(up_away, stats))
    *output, states, slopes = recur(1, place, gate, z, stats, params, valid, x, True)
    other_near = over_c(after(other, slopes))
    saved.append((own_split, (other, other_near), z, stats, states, slopes))
    diagonal = over_c(over_h(output[3]))

    ups = upstream
    results = [None] * LAYERS
    for layer in range(LAYERS - 1, -1, -1):
        own_split, other_split, z, stats, states, slopes = saved[layer]
        weight = half_weights[layer]
        grad_pre, sums = back(layer, place, gate, z, stats, params, ups, states, slopes)
        sums = gather(sums, ("y", "x"))
        if layer == 0:
            come[0] = after(come[0], sums, away, output[1][0])
            later, go = step_of((in_hbm(stay[0]), come[0]), (in_hbm(stay[1]), come[1]))
            sums = after(sums, later)
            go = over_second(go)
        sums = gather(sums, ("h", "c"))
        grad_z, leaving, *terms, sums = norm_back(
            other_columns, place, grad_pre, z, params, valid, stats, sums, weight, layer,
            layer == 0,
        )
        leaving = over_c(leaving)
        if layer > 0:
            received = [swap_half(terms[0])]
            other_split = prepare(place, *after(other_split, grad_z))
            leaving = after(leaving, diagonal, other_split[0])
        else:
            received = [None, swap_half(terms[1])]
            later, go = step_of((later, after(go, grad_z)))
            leaving = after(leaving, later)
            go = lax.ppermute(go, ("h", "c"), DIAGONAL)
            later = (later, go)
        *first, g_high, g_low = weight_rows(0, place, (grad_z, leaving), own_split, width)
        turned = (g_high, g_low)
        come = [plane_swap(first[1], 0)]
        if layer == 0:
            received[0] = swap_half(after(terms[0], received[1]))
        second = weight_rows(1, place, turned, other_split, width)
        come.append(plane_swap(second[1], 0))
        stay = (first[0], second[0])
        kept = own_terms(own_columns, place, after(grad_z, second[0]), ups, weight, layer)
        if layer > 0:
            away = over_h(after(output[2], kept))
            output = [(a, 0) for a in (output[0], over_c(output[1]), away, diagonal)]
        ups = [(kept, None)] + [(r, None) for r in received]
        results[layer] = lax.dynamic_index_in_dim(
            sums.reshape(3, 4, width), clip, axis=1, keepdims=False
        )

    sums = jnp.stack(results)
    sums = [sums[:, 0], sums[:, 1], sums[:, 2]]
    aways = merge(kept, 1, received[1], apart=True)
    later = (later[0], over_c(after(later[1], aways[0])))
    come[0] = after(come[0], sums, later[1])
    far_near = over_c(lax.ppermute(aways[0], ("h", "c"), DIAGONAL))
    near_sum, far_sum, near_go, far_go = step_of(
        (in_hbm(stay[0]), come[0]), (in_hbm(stay[1]), come[1]), cut=2
    )
    near_go, far_go = over_second(near_go), over_second(far_go)
    (go,) = step_of((far_sum, after(far_go, far_near)), cut=0)
    (later,) = step_of(later, cut=0)
    later = after(later, go)
    go = over_h(go)
    later = plane_gather(later)
    (total,) = step_of((near_sum, near_go), cut=0)
    output = unpack(place, [(after(array, total), i) for array, i in output], frames, waited=True)
    close = merge(kept, 0, after(received[0], output))
    far = over_c(over_h(after(aways[1], go)))
    (share,) = step_of((total, after(go, close, *later[1:])), cut=0)
    gathered = plane_gather(share)
    grad_in = [(close, 0), (over_c(close[frames:]), 0), (far_near, 0), (far, 0)]
    grad_in = unpack(place, grad_in, frames)
    grad_weights = assemble(place, after(later, share), 1)
    grad_weights = assemble(place, after(gathered, grad_in), 0, grad_weights)
    return (output, grad_in, grad_weights, *sums, sums[1])


def gelu_slope(value):
    return (
        0.5 * (1.0 + jax.scipy.special.erf(value / ROOT_TWO))
        + value * jnp.exp(-0.5 * value * value) / ROOT_TWO_PI
    )


def recur_step(decay, state, inputs):
    drive_t, valid_t = inputs
    pre = drive_t + decay * state
    state = state + valid_t * (jax.nn.gelu(pre, approximate=False) - state)
    return (state, state)


def back_step(decay, carry, inputs):
    upstream_t, valid_t, pre_t = inputs
    total = upstream_t + carry
    grad_pre = total * valid_t * gelu_slope(pre_t)
    carry = total * (1.0 - valid_t) + grad_pre * decay
    return (carry, grad_pre)


def add_piece(weight, piece):
    return jnp.dot(weight, piece, precision=HIGH, preferred_element_type=jnp.float32)


def weight_columns(grad_pre_norm, piece):
    return jnp.einsum("jf,kf->jk", grad_pre_norm, piece, precision=HIGH)


def split_features(inputs, weights, gains, shifts, decays, biases, lengths, frame_mask, grad_out):
    width, slots = inputs.shape
    clips, frames_len = frame_mask.shape
    frames = jnp.arange(frames_len, dtype=jnp.int32)
    valid_grid = (
        (frames[None, :] < lengths[:, None]) & ((frame_mask == 1) | (frames[None, :] == 0))
    ).astype(jnp.float32)
    valid = valid_grid.reshape(-1)
    valid_row = valid[None, :]
    valid_time = jnp.broadcast_to(valid_grid.T[:, :, None], (frames_len, clips, width)).reshape(
        frames_len, clips * width
    )
    count_local = jnp.sum(valid)

    def to_time(array):
        return jnp.transpose(array.reshape(width, clips, frames_len), (2, 1, 0)).reshape(
            frames_len, clips * width
        )

    def from_time(array):
        return jnp.transpose(array.reshape(frames_len, clips, width), (2, 1, 0)).reshape(
            width, slots
        )

    layer_in = inputs
    saved = []
    for layer_no in range(LAYERS):
        weight = weights[layer_no]
        gathered = lax.all_gather(layer_in, "neuron", axis=0, tiled=True)
        pre_norm = add_piece(weight, gathered)
        first_sum, count = lax.psum((jnp.sum(valid_row * pre_norm, axis=1), count_local), "batch")
        mean = first_sum / count
        centered = pre_norm - mean[:, None]
        var = lax.psum(jnp.sum(valid_row * centered * centered, axis=1), "batch") / count
        inv_std = lax.rsqrt(var + EPS)
        zhat = (pre_norm - mean[:, None]) * inv_std[:, None]
        drive = gains[layer_no][:, None] * zhat + (shifts[layer_no] + biases[layer_no])[:, None]
        drive_time = to_time(drive)
        decay_wide = jnp.tile(decays[layer_no], clips)
        start_state = jnp.zeros((clips * width,), jnp.float32)
        _, states = lax.scan(
            partial(recur_step, decay_wide), start_state, (drive_time, valid_time), unroll=8
        )
        saved.append((gathered, zhat, inv_std, drive_time, states, count))
        layer_in = layer_in + valid_row * from_time(states)
    upstream = grad_out
    grad_parts = [None] * LAYERS
    for layer_no in range(LAYERS - 1, -1, -1):
        gathered, zhat, inv_std, drive_time, states, count = saved[layer_no]
        decay_wide = jnp.tile(decays[layer_no], clips)
        gain = gains[layer_no]
        previous = jnp.concatenate([jnp.zeros_like(states[:1]), states[:-1]], axis=0)
        pre_time = drive_time + decay_wide[None, :] * previous
        grad_state = to_time(valid_row * upstream)
        start_carry = jnp.zeros((clips * width,), jnp.float32)
        _, grad_pre_time = lax.scan(
            partial(back_step, decay_wide),
            start_carry,
            (grad_state, valid_time, pre_time),
            reverse=True,
            unroll=8,
        )
        decay_local = jnp.sum(
            jnp.sum(grad_pre_time * previous, axis=0).reshape(clips, width), axis=0
        )
        grad_pre = from_time(grad_pre_time)
        gain_local = jnp.sum(grad_pre * zhat, axis=1)
        shift_local = jnp.sum(grad_pre, axis=1)
        grad_gain, grad_shift, grad_decay = lax.psum(
            (gain_local, shift_local, decay_local), "batch"
        )
        grad_pre_norm = (gain * inv_std)[:, None] * (
            grad_pre - valid_row * (grad_shift[:, None] + zhat * grad_gain[:, None]) / count
        )
        weight_local = weight_columns(grad_pre_norm, gathered)
        input_terms = jnp.einsum("jk,jf->kf", weights[layer_no], grad_pre_norm, precision=HIGH)
        input_grad = lax.psum_scatter(input_terms, "neuron", scatter_dimension=0, tiled=True)
        grad_weight = lax.psum(weight_local, "batch")
        upstream = upstream + input_grad
        grad_parts[layer_no] = (grad_weight, grad_gain, grad_shift, grad_decay)
    grad_weights = jnp.stack([grad_parts[layer_no][0] for layer_no in range(LAYERS)])
    grad_gains = jnp.stack([grad_parts[layer_no][1] for layer_no in range(LAYERS)])
    grad_shifts = jnp.stack([grad_parts[layer_no][2] for layer_no in range(LAYERS)])
    grad_decays = jnp.stack([grad_parts[layer_no][3] for layer_no in range(LAYERS)])
    return (layer_in, upstream, grad_weights, grad_gains, grad_shifts, grad_decays, grad_shifts)


def solution(mesh):
    if (mesh.shape["batch"], mesh.shape["neuron"]) == (4, 8):
        cut = Mesh(mesh.devices.reshape(2, 2, 2, 2, 2), ("y", "x", "h", "l", "c"))
        batch, neuron, body = ("y", "x"), ("h", "l", "c"), half_features
    else:
        cut, batch, neuron, body = mesh, "batch", "neuron", split_features
    in_specs = (
        P(neuron, batch),
        P(None, neuron, None),
        P(None, neuron),
        P(None, neuron),
        P(None, neuron),
        P(None, neuron),
        P(batch),
        P(batch, None),
        P(neuron, batch),
    )
    out_specs = (
        P(neuron, batch),
        P(neuron, batch),
        P(None, neuron, None),
        P(None, neuron),
        P(None, neuron),
        P(None, neuron),
        P(None, neuron),
    )
    return jax.shard_map(
        body, mesh=cut, in_specs=in_specs, out_specs=out_specs, check_vma=False
    )
```

```python
from functools import partial
import math

import jax
import jax.numpy as jnp
from jax import lax
from jax.experimental import pallas as pl
from jax.experimental.pallas import tpu as pltpu
from jax.sharding import Mesh, PartitionSpec as P

LAYERS = 2
EPS = 1e-05
HIGH = lax.Precision.HIGHEST
ROOT_TWO = math.sqrt(2.0)
ROOT_TWO_PI = math.sqrt(2.0 * math.pi)
F32 = jnp.float32
BF16 = jnp.bfloat16
LANES = 128
VMEM_LIMIT = 24 * 1024 * 1024
SMEM_SPEC = pl.BlockSpec(memory_space=pltpu.SMEM)
VMEM_SPEC = pl.BlockSpec(memory_space=pltpu.VMEM)


FLIP2 = [(0, 1), (1, 0)]
DIAGONAL = [(0, 3), (1, 2), (2, 1), (3, 0)]


def swap_half(array):
    return lax.ppermute(array, "l", FLIP2)


def after(value, *others):
    return lax.optimization_barrier((value, others))[0]


def split(value):
    high = value.astype(BF16)
    return high, (value - high.astype(F32)).astype(BF16)


def dot(a, b, dims):
    return lax.dot_general(a, b, (dims, ((), ())), preferred_element_type=F32)


NT = ((1,), (1,))
NN = ((1,), (0,))


def in_hbm(array):
    return pltpu.with_memory_space_constraint(array, pltpu.HBM)


def call(body, out_shape, hbm_outs=(), **kwargs):
    if hbm_outs:
        out_shape = [
            pltpu.HBM(a.shape, a.dtype) if i in hbm_outs else a for i, a in enumerate(out_shape)
        ]
    return pl.pallas_call(
        body,
        out_shape=out_shape,
        compiler_params=pltpu.CompilerParams(vmem_limit_bytes=VMEM_LIMIT),
        **kwargs,
    )


def cost(flops, byte_count):
    return pl.CostEstimate(flops=int(flops) // 64, bytes_accessed=int(byte_count) // 64, transcendentals=0)


def pack_body(frames, place_ref, in_ref, near_ref, far_ref, turned):
    slots = in_ref.shape[1]
    for start in range(0, slots, LANES):
        turned[start : start + LANES, :] = in_ref[:, start : start + LANES].T
    for rel in range(4):
        first = pl.multiple_of(place_ref[rel] * frames, 8)
        out = (near_ref, far_ref)[rel // 2]
        out[(rel % 2) * frames : (rel % 2 + 1) * frames, :] = turned[pl.ds(first, frames), :]


def pack(place, array, frames, waits=False):
    width, slots = array.shape
    out = jax.ShapeDtypeStruct((2 * frames, width), F32)
    return call(
        partial(pack_body, frames),
        grid=(1,),
        out_shape=[out, out],
        in_specs=[SMEM_SPEC, pl.BlockSpec((width, slots), lambda i: (0, 0))],
        out_specs=[pl.BlockSpec(out.shape, lambda i: (0, 0))] * 2,
        scratch_shapes=[pltpu.VMEM((slots, width), F32)],
        hbm_outs=(0, 1) if waits else (),
        cost_estimate=cost(0, 8 * width * slots),
        name="pack",
    )(place, in_hbm(array))


def part_spec(part, frames):
    array, i = part
    if i is None:
        return pl.BlockSpec(array.shape, lambda *_: (0,) * array.ndim)
    return pl.BlockSpec((frames, array.shape[1]), lambda *_: (i, 0))


def arrays_of(parts):
    return [array for array, _ in parts]


def unpack_body(frames, place_ref, *refs):
    ins, out_ref, turned = refs[:4], refs[4], refs[5]
    slots = out_ref.shape[1]
    for rel in range(4):
        first = pl.multiple_of(place_ref[rel] * frames, 8)
        turned[pl.ds(first, frames), :] = ins[rel][...]
    for start in range(0, slots, LANES):
        out_ref[:, start : start + LANES] = turned[start : start + LANES, :].T


def unpack(place, parts, frames, waited=False):
    width = parts[0][0].shape[1]
    slots = 4 * frames
    return call(
        partial(unpack_body, frames),
        grid=(1,),
        out_shape=jax.ShapeDtypeStruct((width, slots), F32),
        in_specs=[SMEM_SPEC] + [part_spec(part, frames) for part in parts],
        out_specs=pl.BlockSpec((width, slots), lambda i: (0, 0)),
        scratch_shapes=[pltpu.VMEM((slots, width), F32)],
        cost_estimate=cost(0, 8 * width * slots),
        name="unpack",
    )(place, *[in_hbm(a) if waited else a for a in arrays_of(parts)])


def merge_body(kept_ref, come_ref, *outs):
    frames, columns = kept_ref.shape
    width = columns // 2
    for i in range(2):
        some = slice(i * width, (i + 1) * width)
        if len(outs) > 1:
            outs[i][...] = kept_ref[:, some] + come_ref[:, some]
            continue
        (out_ref,) = outs
        out_ref[i * frames : (i + 1) * frames, :] = kept_ref[:, some] + come_ref[:, some]


def merge(kept, half, come, apart=False):
    frames, columns = come.shape
    rows, n = (frames, 2) if apart else (2 * frames, 1)
    outs = call(
        merge_body,
        grid=(1,),
        out_shape=[jax.ShapeDtypeStruct((rows, columns // 2), F32)] * n,
        in_specs=[
            pl.BlockSpec((frames, columns), lambda i: (0, half)),
            pl.BlockSpec((frames, columns), lambda i: (0, 0)),
        ],
        out_specs=[pl.BlockSpec((rows, columns // 2), lambda i: (0, 0))] * n,
        cost_estimate=cost(0, 12 * frames * columns),
        name="merge",
    )(kept, come)
    return outs if apart else outs[0]


def project_body(n_parts, n_flat, spots, n_weights, first, with_acc, with_stats, with_params, cols_ref, place_ref, *refs):
    del cols_ref

    def take(n):
        nonlocal refs
        some, refs = refs[:n], refs[n:]
        return some

    parts, flat_parts, weights = take(n_parts), take(n_flat), take(n_weights)
    acc, valid, stats_in, params = take(with_acc), take(with_stats > 0), take(with_stats > 1), take(with_params)
    (out_ref,) = take(1)
    stats, flat = take(with_stats > 0), take(n_flat > 0)
    x_high, x_low, far_ref = refs
    step = pl.program_id(0)
    width = x_high.shape[2]

    @pl.when(step == 0)
    def _():
        for block, part in zip(spots, parts):
            for start in range(0, part.shape[1], width):
                high, low = split(part[:, start : start + width])
                x_high[block + start // width] = high
                x_low[block + start // width] = low
        column = 0
        for part in flat_parts:
            flat[0][:, column : column + part.shape[1]] = part[...]
            column += part.shape[1]
        if with_acc:
            out_ref[...] = acc[0][...]
        else:
            out_ref[...] = jnp.zeros_like(out_ref)

    stacked = jnp.concatenate([x_high[step], x_low[step], x_high[step]], axis=1)
    for block, weight in enumerate(weight_blocks(place_ref, weights, far_ref)):
        w_high, w_low = split(weight)
        columns = slice(block * width, (block + 1) * width)
        out_ref[:, columns] += dot(stacked, jnp.concatenate([w_high, w_high, w_low], axis=1), NT)

    if with_stats:
        (stats_ref,) = stats

        @pl.when(step == pl.num_programs(0) - 1)
        def _():
            if stats_in:
                stats_ref[...] = stats_in[0][...]
            own = jnp.sum(valid[0][...], axis=0, keepdims=True)
            per = width // LANES
            for row in range(out_ref.shape[1] // LANES):
                z = out_ref[:, row * LANES : (row + 1) * LANES]
                total = jnp.sum(valid[0][...] * z, axis=0, keepdims=True)
                centred = valid[0][...] * (z - total / own)
                squares = jnp.sum(centred * centred, axis=0, keepdims=True)
                at = place_ref[first + row // per] * per + row % per
                stats_ref[0, pl.ds(at, 1), :] = total
                stats_ref[1, pl.ds(at, 1), :] = squares
                stats_ref[2, pl.ds(at, 1), :] = own
            if with_params:
                rest = params[0].shape[0] - 8
                stats_ref[3] = params[0][:8, :]
                stats_ref[4] = jnp.zeros_like(stats_ref[4])
                stats_ref[4, :rest, :] = params[0][8:, :]


def weight_specs(weights, layer, pairs=2):
    specs = []
    for weight in weights:
        if weight.ndim == 3:
            shape = (1, weight.shape[1], pairs * weight.shape[1])
            specs.append(pl.BlockSpec(shape, lambda s, cols, *_: (layer, 0, cols[s])))
        else:
            shape = (weight.shape[0], pairs * 4 * weight.shape[0])
            specs.append(pl.BlockSpec(shape, lambda s, cols, *_: (0, cols[s])))
    return specs


def far_scratch(width, pairs=2):
    return pltpu.VMEM((2, width, pairs * width), F32)


def weight_blocks(place_ref, refs, far_ref):
    near = [ref[0] for ref in refs if len(ref.shape) == 3]
    pieces = [ref for ref in refs if len(ref.shape) == 2]
    far = []
    for i in range(len(pieces) // 4):
        for rel, piece in enumerate(pieces[4 * i : 4 * i + 4]):
            rows = piece.shape[0]
            row = 2 * (place_ref[4] ^ (rel // 2)) + (place_ref[5] ^ (rel % 2))
            far_ref[i, pl.ds(pl.multiple_of(row * rows, rows), rows), :] = piece[...]
        far.append(far_ref[i])
    return near + far


def project(
    place, frames, parts, blocks, weights, layer, acc=None, valid=None, stats=None, params=None, flat=()
):
    near = weights[0].ndim == 3
    units = sum(1 if w.ndim == 3 else 0.25 for w in weights)
    width = weights[0].shape[1] if near else 4 * weights[0].shape[0]
    n = blocks.shape[0]
    spots, block = [], 0
    for array, _ in parts:
        spots.append(block)
        block += array.shape[1] // width
    full = pl.BlockSpec(memory_space=pltpu.VMEM)
    in_specs = [part_spec(part, frames) for part in (*parts, *flat)]
    in_specs += weight_specs(weights, layer, 1)
    operands = arrays_of(parts) + arrays_of(flat) + [in_hbm(w) for w in weights]
    array = jax.ShapeDtypeStruct((frames, int(units) * width), F32)
    array_spec = pl.BlockSpec(array.shape, lambda s, cols, place: (0, 0))
    out_shape, out_specs = [array], [array_spec]
    if acc is not None:
        in_specs.append(array_spec)
        operands.append(in_hbm(acc))
    if valid is not None:
        in_specs.append(full)
        operands.append(valid)
        shape = (3 if params is None else 5, 4 * width // LANES, LANES)
        out_shape.append(jax.ShapeDtypeStruct(shape, F32))
        out_specs.append(pl.BlockSpec(shape, lambda s, cols, place: (0, 0, 0)))
    for extra in (stats, params):
        if extra is not None:
            in_specs.append(full)
            operands.append(extra)
    if flat:
        out_shape.append(jax.ShapeDtypeStruct((frames, 4 * width), F32))
        out_specs.append(pl.BlockSpec((frames, 4 * width), lambda s, cols, place: (0, 0)))
    return call(
        partial(
            project_body,
            len(parts),
            len(flat),
            spots,
            len(weights),
            0 if near else 2,
            acc is not None,
            (valid is not None) + (stats is not None),
            params is not None,
        ),
        grid_spec=pltpu.PrefetchScalarGridSpec(
            num_scalar_prefetch=2,
            grid=(n,),
            in_specs=in_specs,
            out_specs=out_specs,
            scratch_shapes=[pltpu.VMEM((n, frames, width), BF16)] * 2 + [far_scratch(width, 1)],
        ),
        out_shape=out_shape,
        hbm_outs=(0, len(out_shape) - 1) if flat else (0,),
        cost_estimate=cost(6 * frames * n * width * units * width, 4 * n * width * units * width),
        name="project",
    )(blocks, place, *operands)


def to_relative(place_ref, spread, rows_ref, value, slot):
    per = value.shape[0] // 4
    spread[...] = value
    for rel in range(4):
        first = place_ref[rel] * per
        for row in range(per):
            rows_ref[slot, rel * per + row : rel * per + row + 1, :] = spread[
                pl.ds(first + row, 1), :
            ]


def tree(values):
    while len(values) > 1:
        values = [a + b for a, b in zip(values[::2], values[1::2])]
    return values[0]


def gathered(ref, slot):
    return [ref[i] for i in range(slot, ref.shape[0], ref.shape[0] // 16)]


def norm_terms(stats_ref):
    each = [gathered(stats_ref, slot) for slot in range(3)]
    totals, squares, owns = each
    count = tree(owns)
    mean = tree(totals) / count
    away = [total / own - mean for total, own in zip(totals, owns)]
    spread = tree([s + n * a * a for s, n, a in zip(squares, owns, away)])
    return count, mean, lax.rsqrt(spread / count + EPS)


CHUNKS = 4


def columns_of(refs, row):
    for ref in refs:
        if row * LANES < ref.shape[1]:
            return ref[:, row * LANES : (row + 1) * LANES]
        row -= ref.shape[1] // LANES


def recur_body(n_z, last, layer, spread_params, place_ref, gate_ref, *refs):
    z_refs, refs = refs[:n_z], refs[n_z:]
    (stats_ref, params_ref, valid_ref, x_ref), refs = refs[:4], refs[4:]
    outs, refs = refs[: 1 + 3 * last], refs[1 + 3 * last :]
    if spread_params:
        state_ref, slope_ref, params_out, rows, spread, held, drive_s, state_s, slope_s = refs
    else:
        state_ref, slope_ref, rows, spread, held, drive_s, state_s, slope_s = refs
    frames, features = x_ref.shape
    blocks = features // LANES
    per = blocks // 4
    chunk = pl.program_id(0)

    @pl.when(chunk == 0)
    def _():
        if spread_params:
            for rel in range(4):
                first = place_ref[rel] * (stats_ref.shape[0] // 16) + 3
                for row in range(LAYERS * 3 * per):
                    at = rel * per + row % per
                    params_out[row // per, at : at + 1, :] = stats_ref[
                        first + row // 8, row % 8 : row % 8 + 1, :
                    ]
            params = [params_out[3 * layer + i] for i in range(3)]
        else:
            params = [params_ref[3 * layer + i] for i in range(3)]
        _, mean, inv_std = norm_terms(stats_ref)
        to_relative(place_ref, spread, rows, mean, 0)
        to_relative(place_ref, spread, rows, inv_std, 1)
        rows[1] = rows[1] * params[0]
        rows[2] = params[1]
        rows[3] = params[2]
        held[...] = jnp.zeros_like(held)

    for row in range(blocks):
        drive_s[row * frames : (row + 1) * frames, :] = (
            columns_of(z_refs, row) - rows[0, row : row + 1, :]
        ) * rows[1, row : row + 1, :] + rows[2, row : row + 1, :]
    decay = rows[3]

    def step(t, state):
        at = pl.ds(t, blocks, stride=frames)
        pre = drive_s[at, :] + decay * state
        half = 0.5 + 0.5 * lax.erf(pre * (1.0 / ROOT_TWO))
        gate = gate_ref[chunk * frames + t] > 0.0
        slope = half + pre * jnp.exp(-0.5 * pre * pre) * (1.0 / ROOT_TWO_PI)
        state = jnp.where(gate, pre * half, state)
        state_s[at, :] = state
        slope_s[at, :] = jnp.where(gate, slope, 0.0)
        return state

    held[...] = lax.fori_loop(0, frames, step, held[...], unroll=8)
    valid = valid_ref[...]
    for row in range(blocks):
        lanes = slice(row * LANES, (row + 1) * LANES)
        state = state_s[row * frames : (row + 1) * frames, :]
        state_ref[:, lanes] = state
        slope_ref[:, lanes] = slope_s[row * frames : (row + 1) * frames, :]
        value = x_ref[:, lanes] + valid * state
        out, at = (outs[row // per], row % per) if last else (outs[0], row)
        out[:, at * LANES : (at + 1) * LANES] = value


def recur(layer, place, gate, z, stats, params, valid, x, last):
    frames, features = x.shape
    blocks = features // LANES
    some = frames // CHUNKS
    whole = lambda array: pl.BlockSpec(array.shape, lambda i: (0,) * array.ndim)
    by_chunk = lambda array: pl.BlockSpec((some, array.shape[1]), lambda i: (i, 0))
    full = jax.ShapeDtypeStruct((frames, features), F32)
    piece = jax.ShapeDtypeStruct((frames, features // 4), F32)
    out_shape = [piece] * 4 if last else [full]
    out_shape += [full, full]
    out_specs = [by_chunk(a) for a in out_shape]
    spread_params = params is None
    if spread_params:
        out_shape.append(jax.ShapeDtypeStruct((3 * LAYERS, blocks, LANES), F32))
        out_specs.append(whole(out_shape[-1]))
        params = valid
    return call(
        partial(recur_body, len(z), last, layer, spread_params),
        grid=(CHUNKS,),
        in_specs=[SMEM_SPEC, SMEM_SPEC]
        + [by_chunk(a) for a in z]
        + [whole(a) for a in (stats, params)]
        + [by_chunk(a) for a in (valid, x)],
        out_specs=out_specs,
        out_shape=out_shape,
        hbm_outs=tuple(range(len(out_shape) - spread_params)) if last else (1, 2),
        scratch_shapes=[
            pltpu.VMEM((4, blocks, LANES), F32),
            pltpu.VMEM((blocks, LANES), F32),
            pltpu.VMEM((blocks, LANES), F32),
        ]
        + [pltpu.VMEM((blocks * some, LANES), F32)] * 3,
        cost_estimate=cost(100 * frames * features, 20 * frames * features),
        name="recur",
    )(place, gate, *[in_hbm(a) for a in z], stats, params, valid, in_hbm(x))


def back_body(n_z, n_ups, spots, layer, place_ref, gate_ref, *refs):
    z_refs, refs = refs[:n_z], refs[n_z:]
    (stats_ref, params_ref), refs = refs[:2], refs[2:]
    ups, (state_ref, slope_ref), refs = refs[:n_ups], refs[n_ups : n_ups + 2], refs[n_ups + 2 :]
    grad_ref, sums_ref, rows, spread, held, up_s, state_s, slope_s = refs
    frames, features = state_ref.shape
    blocks = features // LANES
    per = blocks // 4
    tall = frames + 8
    step_no = pl.program_id(0)
    chunk = pl.num_programs(0) - 1 - step_no

    @pl.when(step_no == 0)
    def _():
        _, mean, inv_std = norm_terms(stats_ref)
        to_relative(place_ref, spread, rows, mean, 0)
        to_relative(place_ref, spread, rows, inv_std, 1)
        held[...] = jnp.zeros_like(held)

    for row in range(blocks):
        lanes = slice(row * LANES, (row + 1) * LANES)
        base = row * frames
        up = None
        for (_, column), part in zip(spots, ups):
            if column <= row * LANES < column + part.shape[1]:
                value = part[:, row * LANES - column : (row + 1) * LANES - column]
                up = value if up is None else up + value
        up_s[base : base + frames, :] = up
        state_s[row * tall : row * tall + 8, :] = jnp.zeros((8, LANES), F32)
        state_s[row * tall + 8 : (row + 1) * tall, :] = state_ref[:, lanes]
        slope_s[base : base + frames, :] = slope_ref[:, lanes]
    decay = params_ref[3 * layer + 2]

    def step(i, carry):
        t = frames - 1 - i
        at = pl.ds(t, blocks, stride=frames)
        slope = slope_s[at, :]
        gate = gate_ref[chunk * frames + t]
        total = gate * up_s[at, :] + carry
        up_s[at, :] = total * slope
        return total * (slope * decay + (1.0 - gate))

    held[0] = lax.fori_loop(0, frames, step, held[0], unroll=8)
    held[4] += held[1] * state_s[pl.ds(tall - 1, blocks, stride=tall), :]
    held[1] = up_s[pl.ds(0, blocks, stride=frames), :]
    for row in range(blocks):
        lanes = slice(row * LANES, (row + 1) * LANES)
        grad = up_s[row * frames : (row + 1) * frames, :]
        grad_ref[:, lanes] = grad
        zhat = (columns_of(z_refs, row) - rows[0, row : row + 1, :]) * rows[1, row : row + 1, :]
        before = state_s[row * tall + 7 : row * tall + 7 + frames, :]
        for slot, value in enumerate((grad * zhat, grad, grad * before)):
            held[2 + slot, row : row + 1, :] += jnp.sum(value, axis=0, keepdims=True)

    @pl.when(chunk == 0)
    def _():
        for row in range(blocks):
            at = place_ref[row // per] * per + row % per
            for slot in range(3):
                sums_ref[slot, pl.ds(at, 1), :] = held[2 + slot, row : row + 1, :]


def spots_of_sum(parts, width):
    spots, column = [], 0
    for array, _ in parts:
        spots.append((0, column % (4 * width)))
        column += array.shape[1]
    return spots


def back(layer, place, gate, z, stats, params, ups, states, slopes):
    frames, features = states.shape
    width = features // 4
    blocks = features // LANES
    some = frames // CHUNKS
    whole = lambda array: pl.BlockSpec(array.shape, lambda i: (0,) * array.ndim)

    def by_chunk(array, first=0):
        return pl.BlockSpec(
            (some, array.shape[1]), lambda i: ((first or 0) * CHUNKS + CHUNKS - 1 - i, 0)
        )

    out_shape = [
        jax.ShapeDtypeStruct((frames, features), F32),
        jax.ShapeDtypeStruct((3, blocks, LANES), F32),
    ]
    return call(
        partial(back_body, len(z), len(ups), spots_of_sum(ups, width), layer),
        grid=(CHUNKS,),
        in_specs=[SMEM_SPEC] * 2
        + [by_chunk(a) for a in z]
        + [whole(a) for a in (stats, params)]
        + [by_chunk(*up) for up in ups]
        + [by_chunk(a) for a in (states, slopes)],
        out_specs=[by_chunk(out_shape[0]), whole(out_shape[1])],
        out_shape=out_shape,
        scratch_shapes=[
            pltpu.VMEM((2, blocks, LANES), F32),
            pltpu.VMEM((blocks, LANES), F32),
            pltpu.VMEM((5, blocks, LANES), F32),
            pltpu.VMEM((blocks * some, LANES), F32),
            pltpu.VMEM((blocks * (some + 8), LANES), F32),
            pltpu.VMEM((blocks * some, LANES), F32),
        ],
        cost_estimate=cost(30 * frames * features, 20 * frames * features),
        name="back",
    )(
        place,
        gate,
        *[in_hbm(a) for a in z],
        stats,
        params,
        *arrays_of(ups),
        in_hbm(states),
        in_hbm(slopes),
    )


def input_terms(high_s, low_s, weights):
    left, right = [], []
    for block, weight in enumerate(weights):
        w_high, w_low = split(weight)
        left += [high_s[block], low_s[block], high_s[block]]
        right += [w_high, w_high, w_low]
    return dot(jnp.concatenate(left, axis=1), jnp.concatenate(right, axis=0), NN)


def norm_back_body(n_z, split_terms, layer, cols_ref, place_ref, grad_ref, *refs):
    del cols_ref
    z_refs, refs = refs[:n_z], refs[n_z:]
    params_ref, valid_ref, stats_ref, sums_ref, *refs = refs
    weights, refs = refs[:10], refs[10:]
    if split_terms:
        out_ref, leave_ref, near_term_ref, far_term_ref, sums_out_ref, *refs = refs
        term_refs, starts = (far_term_ref, near_term_ref), (0, 0)
    else:
        out_ref, leave_ref, term_ref, sums_out_ref, *refs = refs
        term_refs, starts = (term_ref, term_ref), (2 * grad_ref.shape[1] // 4, 0)
    rows, spread, high_s, low_s, far_ref = refs
    blocks = grad_ref.shape[1] // LANES
    width = high_s.shape[2]
    per = width // LANES

    @pl.when(pl.program_id(0) == 0)
    def _():
        count, mean, inv_std = norm_terms(stats_ref)
        to_relative(place_ref, spread, rows, mean, 0)
        to_relative(place_ref, spread, rows, inv_std, 1)
        rows[2] = rows[1] * params_ref[3 * layer]
        sums = [tree(gathered(sums_ref, slot)) for slot in range(3)]
        for slot in range(3):
            sums_out_ref[slot] = sums[slot]
        to_relative(place_ref, spread, rows, sums[0] / count, 3)
        to_relative(place_ref, spread, rows, sums[1] / count, 4)
        valid = valid_ref[...]
        for row in range(blocks):
            lanes = slice(row * LANES, (row + 1) * LANES)
            one = lambda slot: rows[slot, row : row + 1, :]
            zhat = (columns_of(z_refs, row) - one(0)) * one(1)
            value = one(2) * (grad_ref[:, lanes] - valid * (one(4) + zhat * one(3)))
            out_ref[:, lanes] = value
            if (row // per) % 2:
                at = (row // per // 2) * width + (row % per) * LANES
                leave_ref[:, at : at + LANES] = value
            high, low = split(value)
            inner = slice((row % per) * LANES, (row % per + 1) * LANES)
            high_s[row // per, :, inner] = high
            low_s[row // per, :, inner] = low

    value = input_terms(high_s, low_s, weight_blocks(place_ref, weights, far_ref))
    for step, (term_ref, first) in enumerate(zip(term_refs, starts)):

        @pl.when(pl.program_id(0) == step)
        def _():
            for pair in range(2):
                at = pl.multiple_of(((place_ref[0] & 1) ^ pair) * width, width)
                term_ref[:, pl.ds(first + at, width)] = value[
                    :, pair * width : (pair + 1) * width
                ]


def norm_back(columns, place, grad, z, params, valid, stats, sums, weights, layer, split_terms):
    frames, features = grad.shape
    width = features // 4
    blocks = features // LANES
    whole = lambda array: pl.BlockSpec(array.shape, lambda s, cols, place: (0,) * array.ndim)
    operands = [grad, *[in_hbm(a) for a in z], params, valid, stats, sums]
    full = jax.ShapeDtypeStruct((frames, features), F32)
    half = jax.ShapeDtypeStruct((frames, 2 * width), F32)
    terms = [half, half] if split_terms else [full]
    out_shape = [full, half, *terms, jax.ShapeDtypeStruct((3, blocks, LANES), F32)]
    return call(
        partial(norm_back_body, len(z), split_terms, layer),
        grid_spec=pltpu.PrefetchScalarGridSpec(
            num_scalar_prefetch=2,
            grid=(2,),
            in_specs=[whole(a) for a in operands] + weight_specs(weights, layer),
            out_specs=[whole(a) for a in out_shape],
            scratch_shapes=[
                pltpu.VMEM((5, blocks, LANES), F32),
                pltpu.VMEM((blocks, LANES), F32),
                pltpu.VMEM((4, frames, width), BF16),
                pltpu.VMEM((4, frames, width), BF16),
                far_scratch(width),
            ],
        ),
        out_shape=out_shape,
        hbm_outs=(0,),
        cost_estimate=cost(6 * frames * features * features, 4 * features * features),
        name="norm_back",
    )(columns, place, *operands, *[in_hbm(w) for w in weights])


def own_terms_body(n_ups, spots, cols_ref, place_ref, grad_ref, *refs):
    del cols_ref
    ups, refs = refs[:n_ups], refs[n_ups:]
    weights, refs = refs[:10], refs[10:]
    out_ref, high_s, low_s, far_ref = refs
    width = high_s.shape[2]
    step = pl.program_id(0)

    @pl.when(step == 0)
    def _():
        for block in range(4):
            high, low = split(grad_ref[:, block * width : (block + 1) * width])
            high_s[block] = high
            low_s[block] = low

    value = input_terms(high_s, low_s, weight_blocks(place_ref, weights, far_ref))
    for pair in range(2):
        at = pl.multiple_of(((place_ref[0] & 1) ^ pair) * width, width)
        out_ref[:, pl.ds(at, width)] = value[:, pair * width : (pair + 1) * width]
    for half in range(2):

        @pl.when(step == half)
        def _():
            first = 2 * half * width
            for (_, column), up in zip(spots, ups):
                low = max(column, first)
                high = min(column + up.shape[1], first + 2 * width)
                if low < high:
                    out_ref[:, low - first : high - first] += up[:, low - column : high - column]


def own_terms(columns, place, grad, ups, weights, layer):
    frames, features = grad.shape
    width = features // 4
    whole = lambda array: pl.BlockSpec(array.shape, lambda s, cols, place: (0,) * array.ndim)
    step_block = pl.BlockSpec((frames, 2 * width), lambda s, cols, place: (0, s))
    return call(
        partial(own_terms_body, len(ups), spots_of_sum(ups, width)),
        grid_spec=pltpu.PrefetchScalarGridSpec(
            num_scalar_prefetch=2,
            grid=(2,),
            in_specs=[whole(grad)]
            + [part_spec(up, frames) for up in ups]
            + weight_specs(weights, layer),
            out_specs=step_block,
            scratch_shapes=[pltpu.VMEM((4, frames, width), BF16)] * 2 + [far_scratch(width)],
        ),
        out_shape=jax.ShapeDtypeStruct((frames, features), F32),
        cost_estimate=cost(6 * frames * features * features, 4 * features * features),
        name="own_terms",
    )(columns, place, in_hbm(grad), *arrays_of(ups), *[in_hbm(w) for w in weights])


def prepare_body(lists_ref, place_ref, own_ref, near_ref, high_ref, low_ref):
    del lists_ref
    padded = high_ref.shape[0] // 2
    width = high_ref.shape[1] // 2
    for clip, part in enumerate((own_ref, near_ref)):
        rows = part.shape[0]
        for dc in range(2):
            at = pl.multiple_of((place_ref[6] ^ clip ^ dc) * width, width)
            high, low = split(part[:, dc * width : (dc + 1) * width])
            high_ref[clip * padded : clip * padded + rows, pl.ds(at, width)] = high
            low_ref[clip * padded : clip * padded + rows, pl.ds(at, width)] = low
        zeros = jnp.zeros((padded - rows, 2 * width), BF16)
        high_ref[clip * padded + rows : (clip + 1) * padded, :] = zeros
        low_ref[clip * padded + rows : (clip + 1) * padded, :] = zeros


def prepare(place, own, near):
    frames, features = own.shape
    width = features // 4
    padded = -(-frames // LANES) * LANES
    in_spec = pl.BlockSpec((frames, 2 * width), lambda s, *_: (0, s))
    out = jax.ShapeDtypeStruct((2 * padded, features), BF16)
    out_spec = pl.BlockSpec((2 * padded, 2 * width), lambda s, order, place: (0, order[s]))
    order = jnp.stack([place[0] >> 1, 1 - (place[0] >> 1)])
    return call(
        prepare_body,
        grid_spec=pltpu.PrefetchScalarGridSpec(
            num_scalar_prefetch=2,
            grid=(2,),
            in_specs=[in_spec, in_spec],
            out_specs=[out_spec, out_spec],
        ),
        out_shape=[out, out],
        hbm_outs=(0, 1),
        cost_estimate=cost(0, 16 * frames * features),
        name="prepare",
    )(order, place, in_hbm(own), in_hbm(near))


def product(g_high, g_low, x_high, x_low):
    return dot(g_high, x_high, NN) + (dot(g_high, x_low, NN) + dot(g_low, x_high, NN))


def weight_body(turn, place_ref, *refs):
    if turn:
        grad_ref, near_ref, x_high, x_low, kept, sent, g_high, g_low, t_high, t_low = refs

        @pl.when(pl.program_id(0) == 0)
        def _():
            frames, features = grad_ref.shape
            width = features // 4
            rows = width // 4
            padded = t_high.shape[1] // 2
            t_high[...] = jnp.zeros_like(t_high)
            t_low[...] = jnp.zeros_like(t_low)
            for clip in range(2):
                for dh in range(2):
                    if clip == 0:
                        part = grad_ref[:, 2 * dh * width : (2 * dh + 1) * width]
                    else:
                        part = near_ref[:, dh * width : (dh + 1) * width]
                    high, low = split(part.T)
                    at = (
                        slice(dh * width, (dh + 1) * width),
                        slice(clip * padded, clip * padded + frames),
                    )
                    t_high[at] = high
                    t_low[at] = low
            for group in range(8):
                first, second, dh = group // 4, group // 2 % 2, group % 2
                core = place_ref[6]
                y = place_ref[4] ^ (first * core + second * (1 - core))
                x = place_ref[5] ^ (first * (1 - core) + second * core)
                at = pl.multiple_of(dh * width + (2 * y + x) * rows, rows)
                g_high[group * rows : (group + 1) * rows, :] = t_high[pl.ds(at, rows), :]
                g_low[group * rows : (group + 1) * rows, :] = t_low[pl.ds(at, rows), :]

    else:
        g_high, g_low, x_high, x_low, kept, sent = refs
    half = g_high.shape[0] // 2
    value = product(g_high[...], g_low[...], x_high[...], x_low[...])
    kept[...] = value[:half].reshape(kept.shape)
    sent[...] = value[half:].reshape(sent.shape)


def weight_rows(side, place, grads, x_split, width):
    turn = side == 0
    whole = lambda array: pl.BlockSpec(array.shape, lambda s, place: (0,) * array.ndim)
    x_spec = pl.BlockSpec((x_split[0].shape[0], width), lambda s, place: (0, s))
    shape = (2, 2, width // 4, 4 * width)
    out_shape = [jax.ShapeDtypeStruct(shape, F32)] * 2
    out_specs = [pl.BlockSpec(shape[:3] + (width,), lambda s, place: (0, 0, 0, s))] * 2
    scratch = []
    if turn:
        turned = (2 * width, x_split[0].shape[0])
        out_shape += [jax.ShapeDtypeStruct(turned, BF16)] * 2
        out_specs += [whole(out_shape[-1])] * 2
        scratch = [pltpu.VMEM(turned, BF16)] * 2
    return call(
        partial(weight_body, turn),
        grid_spec=pltpu.PrefetchScalarGridSpec(
            num_scalar_prefetch=1,
            grid=(4,),
            in_specs=[whole(a) for a in grads] + [x_spec] * 2,
            out_specs=out_specs,
            scratch_shapes=scratch,
        ),
        out_shape=out_shape,
        hbm_outs=(0,),
        cost_estimate=cost(12 * x_split[0].shape[0] * width * 4 * width, 4 * 8 * width * width),
        name="weight_rows",
    )(place, *([in_hbm(grads[0]), grads[1]] if turn else grads), *[in_hbm(x) for x in x_split])


def step_body(n, widths, cut, *refs):
    ins, outs = refs[: 2 * n], refs[2 * n :]
    starts = [sum(widths[:i]) for i in range(len(widths))]
    column = 0
    for i in range(n):
        total = ins[2 * i][...] + ins[2 * i + 1][...]
        end = column + total.shape[-1]
        for j, (start, columns) in enumerate(zip(starts, widths)):
            low, high = max(start, column), min(start + columns, end)
            if low < high:
                to = (Ellipsis, slice(low - start, high - start))
                piece = total[..., low - column : high - column]
                pieces = [piece]
                for _ in range(cut):
                    pieces = [half[k] for half in pieces for k in range(2)]
                for k, some in enumerate(pieces):
                    outs[len(pieces) * j + k][to] = some
        column = end


def step_of(*pairs, cut=1, widths=None):
    shape = list(pairs[0][0].shape)
    widths = widths or [sum(pair[0].shape[-1] for pair in pairs)]
    outs = []
    for columns in widths:
        shape[-1] = columns
        outs += [jax.ShapeDtypeStruct(tuple(shape[cut:]), F32)] * 2**cut
    whole = lambda array: pl.BlockSpec(array.shape, lambda i: (0,) * array.ndim)
    operands = [array for pair in pairs for array in pair]
    return call(
        partial(step_body, len(pairs), widths, cut),
        grid=(1,),
        in_specs=[whole(a) for a in operands],
        out_specs=[whole(a) for a in outs],
        out_shape=outs,
        cost_estimate=cost(0, 4 * sum(a.size for a in operands)),
        name="reduction_step",
    )(*operands)


def plane_swap(array, step):
    pairs = []
    for i in range(8):
        over_x = (i % 2 == 0) == (step == 0)
        pairs.append((i, i ^ 2 if over_x else i ^ 4))
    return lax.ppermute(array, ("y", "x", "c"), pairs)


def plane_gather(share, *before):
    first = plane_swap(share, 0)
    second = plane_swap(after(share, first), 1)
    return [share, second, first, plane_swap(after(first, *before), 1)]


def assemble_body(place_ref, *refs):
    out_ref = refs[-1]
    core = place_ref[6]
    rows, columns = refs[0].shape
    quarter = columns // 4
    for i in range(4):
        first, second = i // 2, i % 2
        y = place_ref[4] ^ (first * core + second * (1 - core))
        x = place_ref[5] ^ (first * (1 - core) + second * core)
        at = pl.multiple_of((2 * y + x) * rows, rows)
        for side in range(2):
            for h in range(2):
                to = pl.multiple_of((2 * h + (place_ref[7] ^ side)) * quarter, quarter)
                some = slice((2 * side + h) * quarter, (2 * side + h + 1) * quarter)
                out_ref[0, pl.ds(at, rows), pl.ds(to, quarter)] = refs[i][:, some]


def assemble(place, pieces, layer, onto=None):
    rows, columns = 4 * pieces[0].shape[0], pieces[0].shape[1]
    aliases, extra, extra_specs = {}, [], []
    if onto is not None:
        aliases, extra = {1 + len(pieces): 0}, [onto]
        extra_specs = [pl.BlockSpec(memory_space=pl.ANY)]
    (out,) = call(
        assemble_body,
        grid=(1,),
        out_shape=[jax.ShapeDtypeStruct((LAYERS, rows, columns), F32)],
        hbm_outs=(0,),
        in_specs=[SMEM_SPEC]
        + [pl.BlockSpec(p.shape, lambda i: (0, 0)) for p in pieces]
        + extra_specs,
        out_specs=[pl.BlockSpec((1, rows, columns), lambda i: (layer, 0, 0))],
        input_output_aliases=aliases,
        cost_estimate=cost(0, 8 * rows * columns),
        name="assemble",
    )(place, *[p if extra else in_hbm(p) for p in pieces], *extra)
    return out


def half_features(inputs, weights, gains, shifts, decays, biases, lengths, frame_mask, grad_out):
    width, slots = inputs.shape
    clips, frames = frame_mask.shape
    depth = weights.shape[2]
    blocks = 4 * width // LANES
    y, x, h, l, c = (lax.axis_index(name) for name in ("y", "x", "h", "l", "c"))
    b = 2 * y + x
    numbers = [2 * (h ^ (rel // 2)) + (c ^ (rel % 2)) for rel in range(4)] + [y, x, c, l]
    place = jnp.stack(numbers).astype(jnp.int32)
    own_blocks, other_blocks = (
        jnp.stack(
            [2 * (2 * (h ^ (rel // 2)) + half) + (c ^ (rel % 2)) for rel in range(4)]
        ).astype(jnp.int32)
        for half in (l, 1 - l)
    )
    own_columns = jnp.stack([2 * h + l, 2 * (1 - h) + l]).astype(jnp.int32)
    other_columns = jnp.stack([2 * (1 - h) + 1 - l, 2 * h + 1 - l]).astype(jnp.int32)
    rows = width // 4

    clip = 2 * h + c
    seen = lax.dynamic_index_in_dim(frame_mask, clip, 0, keepdims=False)
    length = lax.dynamic_index_in_dim(lengths, clip, 0, keepdims=False)
    moments = jnp.arange(frames, dtype=jnp.int32)
    gate = ((moments < length) & ((seen == 1) | (moments == 0))).astype(F32)
    valid = jnp.broadcast_to(gate[:, None], (frames, LANES))

    def far_share(layer):
        return lax.dynamic_slice(weights, (layer, b * rows, 0), (1, rows, depth))[0]

    def over_h(array):
        return lax.ppermute(array, "h", FLIP2)

    def over_c(array):
        return lax.ppermute(array, "c", FLIP2)

    def over_second(array):
        return plane_swap(array, 1)

    def four_of(near_rows, far_rows):
        return [
            (near_rows, 0),
            (over_c(near_rows), 1),
            (far_rows, 0),
            (over_c(far_rows), 1),
        ]

    def four_of_plane(share):
        both = lax.ppermute(share, ("y", "x"), DIAGONAL)
        return [share, lax.ppermute(share, "x", FLIP2), lax.ppermute(share, "y", FLIP2), both]

    near = over_c(weights)
    share = far_share(0)
    close, away = pack(place, after(inputs, share), frames)
    share = over_h(share)
    away = over_h(away)
    other_close = swap_half(close)
    up_close, up_away = pack(place, after(grad_out, close), frames, waits=True)
    share = after(share, up_close, valid, near, other_close)
    pieces = four_of_plane(share)
    away = after(away, pieces[1:])
    half_weights = [[weights, near, *pieces, *map(over_c, after(pieces, away))]]
    own = four_of(after(close, away), away)
    other_away = swap_half(away)
    others = [(other_close, 0), (over_c(other_close), 1)]
    params = jnp.stack([gains, shifts + biases, decays], axis=1)
    own_params = params.reshape(LAYERS * 3 * width // LANES, LANES)
    params = None

    def gather(array, axes):
        return lax.all_gather(array, axes, tiled=True)

    weight = half_weights[0]
    early = jnp.concatenate([own_blocks, other_blocks[:2]])
    z, own_flat = project(place, frames, own + others, early, weight, 0, flat=own)
    others += [(other_away, 0), (over_c(after(other_away, z)), 1)]
    z, stats, other_flat = project(
        place,
        frames,
        others[2:],
        other_blocks[2:],
        weight,
        0,
        z,
        valid,
        params=own_params,
        flat=others,
    )
    z = [z]
    stats = gather(stats, ("h", "c"))
    share = over_c(lax.ppermute(after(far_share(1), stats), ("h", "c"), DIAGONAL))
    stats = gather(stats, ("y", "x"))
    x, states, slopes, params = recur(0, place, gate, z, stats, None, valid, own_flat, False)
    own_near, other_near = over_c(after(own_flat, z[0])), over_c(after(other_flat, z[0]))
    x_near = over_c(x)
    own_split = prepare(place, after(own_flat, x_near), own_near)
    other_split = prepare(place, after(other_flat, x_near), other_near)
    saved = [(own_split, other_split, z, stats, states, slopes)]

    pieces = four_of_plane(after(share, slopes, own_near, other_near))
    near = [weights, near]
    other = swap_half(x)
    x_own = after(x, own_split[0], other_split[0])
    z, *_ = project(place, frames, [(x_own, None)], own_blocks, near, 1)
    own_split = prepare(place, after(x, z), x_near)
    far = [*pieces, *map(over_c, after(pieces, own_split[0]))]
    up_away = over_h(after(up_away, other, own_split[0]))
    half_weights.append(near + far)
    z, stats = project(place, frames, [(other, None)], other_blocks, near, 1, z, valid)
    both = jnp.concatenate([own_blocks, other_blocks])
    z_far, stats = project(
        place,
        frames,
        [(x, None), (other, None)],
        both,
        far,
        1,
        None,
        valid,
        stats,
    )
    z = [z, z_far]
    stats = gather(gather(stats, ("y", "x")), ("h", "c"))
    upstream = four_of(up_close, after(up_away, stats))
    *output, states, slopes = recur(1, place, gate, z, stats, params, valid, x, True)
    other_near = over_c(after(other, slopes))
    saved.append((own_split, (other, other_near), z, stats, states, slopes))
    diagonal = over_c(over_h(output[3]))

    ups = upstream
    results = [None] * LAYERS
    for layer in range(LAYERS - 1, -1, -1):
        own_split, other_split, z, stats, states, slopes = saved[layer]
        weight = half_weights[layer]
        grad_pre, sums = back(layer, place, gate, z, stats, params, ups, states, slopes)
        sums = gather(sums, ("y", "x"))
        if layer == 0:
            come[0] = after(come[0], sums, away, output[1][0])
            later, go = step_of((in_hbm(stay[0]), come[0]), (in_hbm(stay[1]), come[1]))
            sums = after(sums, later)
            go = over_second(go)
        sums = gather(sums, ("h", "c"))
        grad_z, leaving, *terms, sums = norm_back(
            other_columns, place, grad_pre, z, params, valid, stats, sums, weight, layer,
            layer == 0,
        )
        leaving = over_c(leaving)
        if layer > 0:
            received = [swap_half(terms[0])]
            other_split = prepare(place, *after(other_split, grad_z))
            leaving = after(leaving, diagonal, other_split[0])
        else:
            received = [None, swap_half(terms[1])]
            later, go = step_of((later, after(go, grad_z)))
            leaving = after(leaving, later)
            go = lax.ppermute(go, ("h", "c"), DIAGONAL)
            later = (later, go)
        *first, g_high, g_low = weight_rows(0, place, (grad_z, leaving), own_split, width)
        turned = (g_high, g_low)
        come = [plane_swap(first[1], 0)]
        if layer == 0:
            received[0] = swap_half(after(terms[0], received[1]))
        second = weight_rows(1, place, turned, other_split, width)
        come.append(plane_swap(second[1], 0))
        stay = (first[0], second[0])
        kept = own_terms(own_columns, place, after(grad_z, second[0]), ups, weight, layer)
        if layer > 0:
            away = over_h(after(output[2], kept))
            output = [(a, 0) for a in (output[0], over_c(output[1]), away, diagonal)]
        ups = [(kept, None)] + [(r, None) for r in received]
        results[layer] = lax.dynamic_index_in_dim(
            sums.reshape(3, 4, width), clip, axis=1, keepdims=False
        )

    sums = jnp.stack(results)
    sums = [sums[:, 0], sums[:, 1], sums[:, 2]]
    aways = merge(kept, 1, received[1], apart=True)
    later = (later[0], over_c(after(later[1], aways[0])))
    come[0] = after(come[0], sums, later[1])
    far_near = over_c(lax.ppermute(aways[0], ("h", "c"), DIAGONAL))
    near_sum, far_sum, near_go, far_go = step_of(
        (in_hbm(stay[0]), come[0]), (in_hbm(stay[1]), come[1]), cut=2
    )
    near_go, far_go = over_second(near_go), over_second(far_go)
    (go,) = step_of((far_sum, after(far_go, far_near)), cut=0)
    (later,) = step_of(later, cut=0)
    later = after(later, go, received[0])
    go = over_h(go)
    later = plane_gather(later)
    (total,) = step_of((near_sum, near_go), cut=0)
    output = unpack(place, [(after(array, total), i) for array, i in output], frames, waited=True)
    close = merge(kept, 0, after(received[0], output))
    far = over_c(over_h(after(aways[1], go)))
    (share,) = step_of((total, after(go, close, *later[1:])), cut=0)
    grad_weights = assemble(place, after(later, share), 1)
    gathered = plane_gather(share, grad_weights)
    grad_in = [(close, 0), (over_c(close[frames:]), 0), (far_near, 0), (far, 0)]
    grad_in = unpack(place, grad_in, frames)
    grad_weights = assemble(place, after(gathered, grad_in), 0, grad_weights)
    return (output, grad_in, grad_weights, *sums, sums[1])


def gelu_slope(value):
    return (
        0.5 * (1.0 + jax.scipy.special.erf(value / ROOT_TWO))
        + value * jnp.exp(-0.5 * value * value) / ROOT_TWO_PI
    )


def recur_step(decay, state, inputs):
    drive_t, valid_t = inputs
    pre = drive_t + decay * state
    state = state + valid_t * (jax.nn.gelu(pre, approximate=False) - state)
    return (state, state)


def back_step(decay, carry, inputs):
    upstream_t, valid_t, pre_t = inputs
    total = upstream_t + carry
    grad_pre = total * valid_t * gelu_slope(pre_t)
    carry = total * (1.0 - valid_t) + grad_pre * decay
    return (carry, grad_pre)


def add_piece(weight, piece):
    return jnp.dot(weight, piece, precision=HIGH, preferred_element_type=jnp.float32)


def weight_columns(grad_pre_norm, piece):
    return jnp.einsum("jf,kf->jk", grad_pre_norm, piece, precision=HIGH)


def split_features(inputs, weights, gains, shifts, decays, biases, lengths, frame_mask, grad_out):
    width, slots = inputs.shape
    clips, frames_len = frame_mask.shape
    frames = jnp.arange(frames_len, dtype=jnp.int32)
    valid_grid = (
        (frames[None, :] < lengths[:, None]) & ((frame_mask == 1) | (frames[None, :] == 0))
    ).astype(jnp.float32)
    valid = valid_grid.reshape(-1)
    valid_row = valid[None, :]
    valid_time = jnp.broadcast_to(valid_grid.T[:, :, None], (frames_len, clips, width)).reshape(
        frames_len, clips * width
    )
    count_local = jnp.sum(valid)

    def to_time(array):
        return jnp.transpose(array.reshape(width, clips, frames_len), (2, 1, 0)).reshape(
            frames_len, clips * width
        )

    def from_time(array):
        return jnp.transpose(array.reshape(frames_len, clips, width), (2, 1, 0)).reshape(
            width, slots
        )

    layer_in = inputs
    saved = []
    for layer_no in range(LAYERS):
        weight = weights[layer_no]
        gathered = lax.all_gather(layer_in, "neuron", axis=0, tiled=True)
        pre_norm = add_piece(weight, gathered)
        first_sum, count = lax.psum((jnp.sum(valid_row * pre_norm, axis=1), count_local), "batch")
        mean = first_sum / count
        centered = pre_norm - mean[:, None]
        var = lax.psum(jnp.sum(valid_row * centered * centered, axis=1), "batch") / count
        inv_std = lax.rsqrt(var + EPS)
        zhat = (pre_norm - mean[:, None]) * inv_std[:, None]
        drive = gains[layer_no][:, None] * zhat + (shifts[layer_no] + biases[layer_no])[:, None]
        drive_time = to_time(drive)
        decay_wide = jnp.tile(decays[layer_no], clips)
        start_state = jnp.zeros((clips * width,), jnp.float32)
        _, states = lax.scan(
            partial(recur_step, decay_wide), start_state, (drive_time, valid_time), unroll=8
        )
        saved.append((gathered, zhat, inv_std, drive_time, states, count))
        layer_in = layer_in + valid_row * from_time(states)
    upstream = grad_out
    grad_parts = [None] * LAYERS
    for layer_no in range(LAYERS - 1, -1, -1):
        gathered, zhat, inv_std, drive_time, states, count = saved[layer_no]
        decay_wide = jnp.tile(decays[layer_no], clips)
        gain = gains[layer_no]
        previous = jnp.concatenate([jnp.zeros_like(states[:1]), states[:-1]], axis=0)
        pre_time = drive_time + decay_wide[None, :] * previous
        grad_state = to_time(valid_row * upstream)
        start_carry = jnp.zeros((clips * width,), jnp.float32)
        _, grad_pre_time = lax.scan(
            partial(back_step, decay_wide),
            start_carry,
            (grad_state, valid_time, pre_time),
            reverse=True,
            unroll=8,
        )
        decay_local = jnp.sum(
            jnp.sum(grad_pre_time * previous, axis=0).reshape(clips, width), axis=0
        )
        grad_pre = from_time(grad_pre_time)
        gain_local = jnp.sum(grad_pre * zhat, axis=1)
        shift_local = jnp.sum(grad_pre, axis=1)
        grad_gain, grad_shift, grad_decay = lax.psum(
            (gain_local, shift_local, decay_local), "batch"
        )
        grad_pre_norm = (gain * inv_std)[:, None] * (
            grad_pre - valid_row * (grad_shift[:, None] + zhat * grad_gain[:, None]) / count
        )
        weight_local = weight_columns(grad_pre_norm, gathered)
        input_terms = jnp.einsum("jk,jf->kf", weights[layer_no], grad_pre_norm, precision=HIGH)
        input_grad = lax.psum_scatter(input_terms, "neuron", scatter_dimension=0, tiled=True)
        grad_weight = lax.psum(weight_local, "batch")
        upstream = upstream + input_grad
        grad_parts[layer_no] = (grad_weight, grad_gain, grad_shift, grad_decay)
    grad_weights = jnp.stack([grad_parts[layer_no][0] for layer_no in range(LAYERS)])
    grad_gains = jnp.stack([grad_parts[layer_no][1] for layer_no in range(LAYERS)])
    grad_shifts = jnp.stack([grad_parts[layer_no][2] for layer_no in range(LAYERS)])
    grad_decays = jnp.stack([grad_parts[layer_no][3] for layer_no in range(LAYERS)])
    return (layer_in, upstream, grad_weights, grad_gains, grad_shifts, grad_decays, grad_shifts)


def solution(mesh):
    if (mesh.shape["batch"], mesh.shape["neuron"]) == (4, 8):
        cut = Mesh(mesh.devices.reshape(2, 2, 2, 2, 2), ("y", "x", "h", "l", "c"))
        batch, neuron, body = ("y", "x"), ("h", "l", "c"), half_features
    else:
        cut, batch, neuron, body = mesh, "batch", "neuron", split_features
    in_specs = (
        P(neuron, batch),
        P(None, neuron, None),
        P(None, neuron),
        P(None, neuron),
        P(None, neuron),
        P(None, neuron),
        P(batch),
        P(batch, None),
        P(neuron, batch),
    )
    out_specs = (
        P(neuron, batch),
        P(neuron, batch),
        P(None, neuron, None),
        P(None, neuron),
        P(None, neuron),
        P(None, neuron),
        P(None, neuron),
    )
    return jax.shard_map(
        body, mesh=cut, in_specs=in_specs, out_specs=out_specs, check_vma=False
    )
```

```python
from functools import partial
import math

import jax
import jax.numpy as jnp
from jax import lax
from jax.experimental import pallas as pl
from jax.experimental.pallas import tpu as pltpu
from jax.sharding import Mesh, PartitionSpec as P

LAYERS = 2
EPS = 1e-05
HIGH = lax.Precision.HIGHEST
ROOT_TWO = math.sqrt(2.0)
ROOT_TWO_PI = math.sqrt(2.0 * math.pi)
F32 = jnp.float32
BF16 = jnp.bfloat16
LANES = 128
VMEM_LIMIT = 24 * 1024 * 1024
SMEM_SPEC = pl.BlockSpec(memory_space=pltpu.SMEM)
VMEM_SPEC = pl.BlockSpec(memory_space=pltpu.VMEM)


FLIP2 = [(0, 1), (1, 0)]
DIAGONAL = [(0, 3), (1, 2), (2, 1), (3, 0)]


def swap_half(array):
    return lax.ppermute(array, "l", FLIP2)


def after(value, *others):
    return lax.optimization_barrier((value, others))[0]


def split(value):
    high = value.astype(BF16)
    return high, (value - high.astype(F32)).astype(BF16)


def dot(a, b, dims):
    return lax.dot_general(a, b, (dims, ((), ())), preferred_element_type=F32)


NT = ((1,), (1,))
NN = ((1,), (0,))


def in_hbm(array):
    return pltpu.with_memory_space_constraint(array, pltpu.HBM)


def call(body, out_shape, hbm_outs=(), **kwargs):
    if hbm_outs:
        out_shape = [
            pltpu.HBM(a.shape, a.dtype) if i in hbm_outs else a for i, a in enumerate(out_shape)
        ]
    return pl.pallas_call(
        body,
        out_shape=out_shape,
        compiler_params=pltpu.CompilerParams(vmem_limit_bytes=VMEM_LIMIT),
        **kwargs,
    )


def cost(flops, byte_count):
    return pl.CostEstimate(flops=int(flops) // 64, bytes_accessed=int(byte_count) // 64, transcendentals=0)


def pack_body(frames, place_ref, in_ref, near_ref, far_ref, turned):
    slots = in_ref.shape[1]
    for start in range(0, slots, LANES):
        turned[start : start + LANES, :] = in_ref[:, start : start + LANES].T
    for rel in range(4):
        first = pl.multiple_of(place_ref[rel] * frames, 8)
        out = (near_ref, far_ref)[rel // 2]
        out[(rel % 2) * frames : (rel % 2 + 1) * frames, :] = turned[pl.ds(first, frames), :]


def pack(place, array, frames, waits=False):
    width, slots = array.shape
    out = jax.ShapeDtypeStruct((2 * frames, width), F32)
    return call(
        partial(pack_body, frames),
        grid=(1,),
        out_shape=[out, out],
        in_specs=[SMEM_SPEC, pl.BlockSpec((width, slots), lambda i: (0, 0))],
        out_specs=[pl.BlockSpec(out.shape, lambda i: (0, 0))] * 2,
        scratch_shapes=[pltpu.VMEM((slots, width), F32)],
        hbm_outs=(0, 1) if waits else (),
        cost_estimate=cost(0, 8 * width * slots),
        name="pack",
    )(place, in_hbm(array))


def part_spec(part, frames):
    array, i = part
    if i is None:
        return pl.BlockSpec(array.shape, lambda *_: (0,) * array.ndim)
    return pl.BlockSpec((frames, array.shape[1]), lambda *_: (i, 0))


def arrays_of(parts):
    return [array for array, _ in parts]


def unpack_body(frames, place_ref, *refs):
    ins, out_ref, turned = refs[:4], refs[4], refs[5]
    slots = out_ref.shape[1]
    for rel in range(4):
        first = pl.multiple_of(place_ref[rel] * frames, 8)
        turned[pl.ds(first, frames), :] = ins[rel][...]
    for start in range(0, slots, LANES):
        out_ref[:, start : start + LANES] = turned[start : start + LANES, :].T


def unpack(place, parts, frames, waited=False):
    width = parts[0][0].shape[1]
    slots = 4 * frames
    return call(
        partial(unpack_body, frames),
        grid=(1,),
        out_shape=jax.ShapeDtypeStruct((width, slots), F32),
        in_specs=[SMEM_SPEC] + [part_spec(part, frames) for part in parts],
        out_specs=pl.BlockSpec((width, slots), lambda i: (0, 0)),
        scratch_shapes=[pltpu.VMEM((slots, width), F32)],
        cost_estimate=cost(0, 8 * width * slots),
        name="unpack",
    )(place, *[in_hbm(a) if waited else a for a in arrays_of(parts)])


def merge_body(kept_ref, come_ref, *outs):
    frames, columns = kept_ref.shape
    width = columns // 2
    for i in range(2):
        some = slice(i * width, (i + 1) * width)
        if len(outs) > 1:
            outs[i][...] = kept_ref[:, some] + come_ref[:, some]
            continue
        (out_ref,) = outs
        out_ref[i * frames : (i + 1) * frames, :] = kept_ref[:, some] + come_ref[:, some]


def merge(kept, half, come, apart=False):
    frames, columns = come.shape
    rows, n = (frames, 2) if apart else (2 * frames, 1)
    outs = call(
        merge_body,
        grid=(1,),
        out_shape=[jax.ShapeDtypeStruct((rows, columns // 2), F32)] * n,
        in_specs=[
            pl.BlockSpec((frames, columns), lambda i: (0, half)),
            pl.BlockSpec((frames, columns), lambda i: (0, 0)),
        ],
        out_specs=[pl.BlockSpec((rows, columns // 2), lambda i: (0, 0))] * n,
        cost_estimate=cost(0, 12 * frames * columns),
        name="merge",
    )(kept, come)
    return outs if apart else outs[0]


def project_body(n_parts, n_flat, spots, n_weights, first, with_acc, with_stats, with_params, cols_ref, place_ref, *refs):
    del cols_ref

    def take(n):
        nonlocal refs
        some, refs = refs[:n], refs[n:]
        return some

    parts, flat_parts, weights = take(n_parts), take(n_flat), take(n_weights)
    acc, valid, stats_in, params = take(with_acc), take(with_stats > 0), take(with_stats > 1), take(with_params)
    (out_ref,) = take(1)
    stats, flat = take(with_stats > 0), take(n_flat > 0)
    x_high, x_low, far_ref = refs
    step = pl.program_id(0)
    width = x_high.shape[2]

    @pl.when(step == 0)
    def _():
        for block, part in zip(spots, parts):
            for start in range(0, part.shape[1], width):
                high, low = split(part[:, start : start + width])
                x_high[block + start // width] = high
                x_low[block + start // width] = low
        column = 0
        for part in flat_parts:
            flat[0][:, column : column + part.shape[1]] = part[...]
            column += part.shape[1]
        if with_acc:
            out_ref[...] = acc[0][...]
        else:
            out_ref[...] = jnp.zeros_like(out_ref)

    stacked = jnp.concatenate([x_high[step], x_low[step], x_high[step]], axis=1)
    for block, weight in enumerate(weight_blocks(place_ref, weights, far_ref)):
        w_high, w_low = split(weight)
        columns = slice(block * width, (block + 1) * width)
        out_ref[:, columns] += dot(stacked, jnp.concatenate([w_high, w_high, w_low], axis=1), NT)

    if with_stats:
        (stats_ref,) = stats

        @pl.when(step == pl.num_programs(0) - 1)
        def _():
            if stats_in:
                stats_ref[...] = stats_in[0][...]
            own = jnp.sum(valid[0][...], axis=0, keepdims=True)
            per = width // LANES
            for row in range(out_ref.shape[1] // LANES):
                z = out_ref[:, row * LANES : (row + 1) * LANES]
                total = jnp.sum(valid[0][...] * z, axis=0, keepdims=True)
                centred = valid[0][...] * (z - total / own)
                squares = jnp.sum(centred * centred, axis=0, keepdims=True)
                at = place_ref[first + row // per] * per + row % per
                stats_ref[0, pl.ds(at, 1), :] = total
                stats_ref[1, pl.ds(at, 1), :] = squares
                stats_ref[2, pl.ds(at, 1), :] = own
            if with_params:
                rest = params[0].shape[0] - 8
                stats_ref[3] = params[0][:8, :]
                stats_ref[4] = jnp.zeros_like(stats_ref[4])
                stats_ref[4, :rest, :] = params[0][8:, :]


def weight_specs(weights, layer, pairs=2):
    specs = []
    for weight in weights:
        if weight.ndim == 3:
            shape = (1, weight.shape[1], pairs * weight.shape[1])
            specs.append(pl.BlockSpec(shape, lambda s, cols, *_: (layer, 0, cols[s])))
        else:
            shape = (weight.shape[0], pairs * 4 * weight.shape[0])
            specs.append(pl.BlockSpec(shape, lambda s, cols, *_: (0, cols[s])))
    return specs


def far_scratch(width, pairs=2):
    return pltpu.VMEM((2, width, pairs * width), F32)


def weight_blocks(place_ref, refs, far_ref):
    near = [ref[0] for ref in refs if len(ref.shape) == 3]
    pieces = [ref for ref in refs if len(ref.shape) == 2]
    far = []
    for i in range(len(pieces) // 4):
        for rel, piece in enumerate(pieces[4 * i : 4 * i + 4]):
            rows = piece.shape[0]
            row = 2 * (place_ref[4] ^ (rel // 2)) + (place_ref[5] ^ (rel % 2))
            far_ref[i, pl.ds(pl.multiple_of(row * rows, rows), rows), :] = piece[...]
        far.append(far_ref[i])
    return near + far


def project(
    place, frames, parts, blocks, weights, layer, acc=None, valid=None, stats=None, params=None, flat=()
):
    near = weights[0].ndim == 3
    units = sum(1 if w.ndim == 3 else 0.25 for w in weights)
    width = weights[0].shape[1] if near else 4 * weights[0].shape[0]
    n = blocks.shape[0]
    spots, block = [], 0
    for array, _ in parts:
        spots.append(block)
        block += array.shape[1] // width
    full = pl.BlockSpec(memory_space=pltpu.VMEM)
    in_specs = [part_spec(part, frames) for part in (*parts, *flat)]
    in_specs += weight_specs(weights, layer, 1)
    operands = arrays_of(parts) + arrays_of(flat) + [in_hbm(w) for w in weights]
    array = jax.ShapeDtypeStruct((frames, int(units) * width), F32)
    array_spec = pl.BlockSpec(array.shape, lambda s, cols, place: (0, 0))
    out_shape, out_specs = [array], [array_spec]
    if acc is not None:
        in_specs.append(array_spec)
        operands.append(in_hbm(acc))
    if valid is not None:
        in_specs.append(full)
        operands.append(valid)
        shape = (3 if params is None else 5, 4 * width // LANES, LANES)
        out_shape.append(jax.ShapeDtypeStruct(shape, F32))
        out_specs.append(pl.BlockSpec(shape, lambda s, cols, place: (0, 0, 0)))
    for extra in (stats, params):
        if extra is not None:
            in_specs.append(full)
            operands.append(extra)
    if flat:
        out_shape.append(jax.ShapeDtypeStruct((frames, 4 * width), F32))
        out_specs.append(pl.BlockSpec((frames, 4 * width), lambda s, cols, place: (0, 0)))
    return call(
        partial(
            project_body,
            len(parts),
            len(flat),
            spots,
            len(weights),
            0 if near else 2,
            acc is not None,
            (valid is not None) + (stats is not None),
            params is not None,
        ),
        grid_spec=pltpu.PrefetchScalarGridSpec(
            num_scalar_prefetch=2,
            grid=(n,),
            in_specs=in_specs,
            out_specs=out_specs,
            scratch_shapes=[pltpu.VMEM((n, frames, width), BF16)] * 2 + [far_scratch(width, 1)],
        ),
        out_shape=out_shape,
        hbm_outs=(0, len(out_shape) - 1) if flat else (0,),
        cost_estimate=cost(6 * frames * n * width * units * width, 4 * n * width * units * width),
        name="project",
    )(blocks, place, *operands)


def to_relative(place_ref, spread, rows_ref, value, slot):
    per = value.shape[0] // 4
    spread[...] = value
    for rel in range(4):
        first = place_ref[rel] * per
        for row in range(per):
            rows_ref[slot, rel * per + row : rel * per + row + 1, :] = spread[
                pl.ds(first + row, 1), :
            ]


def tree(values):
    while len(values) > 1:
        values = [a + b for a, b in zip(values[::2], values[1::2])]
    return values[0]


def gathered(ref, slot):
    return [ref[i] for i in range(slot, ref.shape[0], ref.shape[0] // 16)]


def norm_terms(stats_ref):
    each = [gathered(stats_ref, slot) for slot in range(3)]
    totals, squares, owns = each
    count = tree(owns)
    mean = tree(totals) / count
    away = [total / own - mean for total, own in zip(totals, owns)]
    spread = tree([s + n * a * a for s, n, a in zip(squares, owns, away)])
    return count, mean, lax.rsqrt(spread / count + EPS)


CHUNKS = 4


def columns_of(refs, row):
    for ref in refs:
        if row * LANES < ref.shape[1]:
            return ref[:, row * LANES : (row + 1) * LANES]
        row -= ref.shape[1] // LANES


def recur_body(n_z, last, layer, spread_params, place_ref, gate_ref, *refs):
    z_refs, refs = refs[:n_z], refs[n_z:]
    (stats_ref, params_ref, valid_ref, x_ref), refs = refs[:4], refs[4:]
    outs, refs = refs[: 1 + 3 * last], refs[1 + 3 * last :]
    if spread_params:
        state_ref, slope_ref, params_out, rows, spread, held, drive_s, state_s, slope_s = refs
    else:
        state_ref, slope_ref, rows, spread, held, drive_s, state_s, slope_s = refs
    frames, features = x_ref.shape
    blocks = features // LANES
    per = blocks // 4
    chunk = pl.program_id(0)

    @pl.when(chunk == 0)
    def _():
        if spread_params:
            for rel in range(4):
                first = place_ref[rel] * (stats_ref.shape[0] // 4) + 3
                for row in range(LAYERS * 3 * per):
                    at = rel * per + row % per
                    params_out[row // per, at : at + 1, :] = stats_ref[
                        first + row // 8, row % 8 : row % 8 + 1, :
                    ]
            params = [params_out[3 * layer + i] for i in range(3)]
        else:
            params = [params_ref[3 * layer + i] for i in range(3)]
        _, mean, inv_std = norm_terms(stats_ref)
        to_relative(place_ref, spread, rows, mean, 0)
        to_relative(place_ref, spread, rows, inv_std, 1)
        rows[1] = rows[1] * params[0]
        rows[2] = params[1]
        rows[3] = params[2]
        held[...] = jnp.zeros_like(held)

    for row in range(blocks):
        drive_s[row * frames : (row + 1) * frames, :] = (
            columns_of(z_refs, row) - rows[0, row : row + 1, :]
        ) * rows[1, row : row + 1, :] + rows[2, row : row + 1, :]
    decay = rows[3]

    def step(t, state):
        at = pl.ds(t, blocks, stride=frames)
        pre = drive_s[at, :] + decay * state
        half = 0.5 + 0.5 * lax.erf(pre * (1.0 / ROOT_TWO))
        gate = gate_ref[chunk * frames + t] > 0.0
        slope = half + pre * jnp.exp(-0.5 * pre * pre) * (1.0 / ROOT_TWO_PI)
        state = jnp.where(gate, pre * half, state)
        state_s[at, :] = state
        slope_s[at, :] = jnp.where(gate, slope, 0.0)
        return state

    held[...] = lax.fori_loop(0, frames, step, held[...], unroll=8)
    valid = valid_ref[...]
    for row in range(blocks):
        lanes = slice(row * LANES, (row + 1) * LANES)
        state = state_s[row * frames : (row + 1) * frames, :]
        state_ref[:, lanes] = state
        slope_ref[:, lanes] = slope_s[row * frames : (row + 1) * frames, :]
        value = x_ref[:, lanes] + valid * state
        out, at = (outs[row // per], row % per) if last else (outs[0], row)
        out[:, at * LANES : (at + 1) * LANES] = value


def recur(layer, place, gate, z, stats, params, valid, x, last):
    frames, features = x.shape
    blocks = features // LANES
    some = frames // CHUNKS
    whole = lambda array: pl.BlockSpec(array.shape, lambda i: (0,) * array.ndim)
    by_chunk = lambda array: pl.BlockSpec((some, array.shape[1]), lambda i: (i, 0))
    full = jax.ShapeDtypeStruct((frames, features), F32)
    piece = jax.ShapeDtypeStruct((frames, features // 4), F32)
    out_shape = [piece] * 4 if last else [full]
    out_shape += [full, full]
    out_specs = [by_chunk(a) for a in out_shape]
    spread_params = params is None
    if spread_params:
        out_shape.append(jax.ShapeDtypeStruct((3 * LAYERS, blocks, LANES), F32))
        out_specs.append(whole(out_shape[-1]))
        params = valid
    return call(
        partial(recur_body, len(z), last, layer, spread_params),
        grid=(CHUNKS,),
        in_specs=[SMEM_SPEC, SMEM_SPEC]
        + [by_chunk(a) for a in z]
        + [whole(a) for a in (stats, params)]
        + [by_chunk(a) for a in (valid, x)],
        out_specs=out_specs,
        out_shape=out_shape,
        hbm_outs=tuple(range(len(out_shape) - spread_params)) if last else (1, 2),
        scratch_shapes=[
            pltpu.VMEM((4, blocks, LANES), F32),
            pltpu.VMEM((blocks, LANES), F32),
            pltpu.VMEM((blocks, LANES), F32),
        ]
        + [pltpu.VMEM((blocks * some, LANES), F32)] * 3,
        cost_estimate=cost(100 * frames * features, 20 * frames * features),
        name="recur",
    )(place, gate, *[in_hbm(a) for a in z], stats, params, valid, in_hbm(x))


def back_body(n_z, n_ups, spots, layer, place_ref, gate_ref, *refs):
    z_refs, refs = refs[:n_z], refs[n_z:]
    (stats_ref, params_ref), refs = refs[:2], refs[2:]
    ups, (state_ref, slope_ref), refs = refs[:n_ups], refs[n_ups : n_ups + 2], refs[n_ups + 2 :]
    grad_ref, sums_ref, rows, spread, held, up_s, state_s, slope_s = refs
    frames, features = state_ref.shape
    blocks = features // LANES
    per = blocks // 4
    tall = frames + 8
    step_no = pl.program_id(0)
    chunk = pl.num_programs(0) - 1 - step_no

    @pl.when(step_no == 0)
    def _():
        _, mean, inv_std = norm_terms(stats_ref)
        to_relative(place_ref, spread, rows, mean, 0)
        to_relative(place_ref, spread, rows, inv_std, 1)
        held[...] = jnp.zeros_like(held)

    for row in range(blocks):
        lanes = slice(row * LANES, (row + 1) * LANES)
        base = row * frames
        up = None
        for (_, column), part in zip(spots, ups):
            if column <= row * LANES < column + part.shape[1]:
                value = part[:, row * LANES - column : (row + 1) * LANES - column]
                up = value if up is None else up + value
        up_s[base : base + frames, :] = up
        state_s[row * tall : row * tall + 8, :] = jnp.zeros((8, LANES), F32)
        state_s[row * tall + 8 : (row + 1) * tall, :] = state_ref[:, lanes]
        slope_s[base : base + frames, :] = slope_ref[:, lanes]
    decay = params_ref[3 * layer + 2]

    def step(i, carry):
        t = frames - 1 - i
        at = pl.ds(t, blocks, stride=frames)
        slope = slope_s[at, :]
        gate = gate_ref[chunk * frames + t]
        total = gate * up_s[at, :] + carry
        up_s[at, :] = total * slope
        return total * (slope * decay + (1.0 - gate))

    held[0] = lax.fori_loop(0, frames, step, held[0], unroll=8)
    held[4] += held[1] * state_s[pl.ds(tall - 1, blocks, stride=tall), :]
    held[1] = up_s[pl.ds(0, blocks, stride=frames), :]
    for row in range(blocks):
        lanes = slice(row * LANES, (row + 1) * LANES)
        grad = up_s[row * frames : (row + 1) * frames, :]
        grad_ref[:, lanes] = grad
        zhat = (columns_of(z_refs, row) - rows[0, row : row + 1, :]) * rows[1, row : row + 1, :]
        before = state_s[row * tall + 7 : row * tall + 7 + frames, :]
        for slot, value in enumerate((grad * zhat, grad, grad * before)):
            held[2 + slot, row : row + 1, :] += jnp.sum(value, axis=0, keepdims=True)

    @pl.when(chunk == 0)
    def _():
        for row in range(blocks):
            at = place_ref[row // per] * per + row % per
            for slot in range(3):
                sums_ref[slot, pl.ds(at, 1), :] = held[2 + slot, row : row + 1, :]


def spots_of_sum(parts, width):
    spots, column = [], 0
    for array, _ in parts:
        spots.append((0, column % (4 * width)))
        column += array.shape[1]
    return spots


def back(layer, place, gate, z, stats, params, ups, states, slopes):
    frames, features = states.shape
    width = features // 4
    blocks = features // LANES
    some = frames // CHUNKS
    whole = lambda array: pl.BlockSpec(array.shape, lambda i: (0,) * array.ndim)

    def by_chunk(array, first=0):
        return pl.BlockSpec(
            (some, array.shape[1]), lambda i: ((first or 0) * CHUNKS + CHUNKS - 1 - i, 0)
        )

    out_shape = [
        jax.ShapeDtypeStruct((frames, features), F32),
        jax.ShapeDtypeStruct((3, blocks, LANES), F32),
    ]
    return call(
        partial(back_body, len(z), len(ups), spots_of_sum(ups, width), layer),
        grid=(CHUNKS,),
        in_specs=[SMEM_SPEC] * 2
        + [by_chunk(a) for a in z]
        + [whole(a) for a in (stats, params)]
        + [by_chunk(*up) for up in ups]
        + [by_chunk(a) for a in (states, slopes)],
        out_specs=[by_chunk(out_shape[0]), whole(out_shape[1])],
        out_shape=out_shape,
        scratch_shapes=[
            pltpu.VMEM((2, blocks, LANES), F32),
            pltpu.VMEM((blocks, LANES), F32),
            pltpu.VMEM((5, blocks, LANES), F32),
            pltpu.VMEM((blocks * some, LANES), F32),
            pltpu.VMEM((blocks * (some + 8), LANES), F32),
            pltpu.VMEM((blocks * some, LANES), F32),
        ],
        cost_estimate=cost(30 * frames * features, 20 * frames * features),
        name="back",
    )(
        place,
        gate,
        *[in_hbm(a) for a in z],
        stats,
        params,
        *arrays_of(ups),
        in_hbm(states),
        in_hbm(slopes),
    )


def input_terms(high_s, low_s, weights):
    left, right = [], []
    for block, weight in enumerate(weights):
        w_high, w_low = split(weight)
        left += [high_s[block], low_s[block], high_s[block]]
        right += [w_high, w_high, w_low]
    return dot(jnp.concatenate(left, axis=1), jnp.concatenate(right, axis=0), NN)


def norm_back_body(n_z, split_terms, layer, cols_ref, place_ref, grad_ref, *refs):
    del cols_ref
    z_refs, refs = refs[:n_z], refs[n_z:]
    params_ref, valid_ref, stats_ref, sums_ref, *refs = refs
    weights, refs = refs[:10], refs[10:]
    if split_terms:
        out_ref, leave_ref, near_term_ref, far_term_ref, sums_out_ref, *refs = refs
        term_refs, starts = (far_term_ref, near_term_ref), (0, 0)
    else:
        out_ref, leave_ref, term_ref, sums_out_ref, *refs = refs
        term_refs, starts = (term_ref, term_ref), (2 * grad_ref.shape[1] // 4, 0)
    rows, spread, high_s, low_s, far_ref = refs
    blocks = grad_ref.shape[1] // LANES
    width = high_s.shape[2]
    per = width // LANES

    @pl.when(pl.program_id(0) == 0)
    def _():
        count, mean, inv_std = norm_terms(stats_ref)
        to_relative(place_ref, spread, rows, mean, 0)
        to_relative(place_ref, spread, rows, inv_std, 1)
        rows[2] = rows[1] * params_ref[3 * layer]
        sums = [tree(gathered(sums_ref, slot)) for slot in range(3)]
        for slot in range(3):
            sums_out_ref[slot] = sums[slot]
        to_relative(place_ref, spread, rows, sums[0] / count, 3)
        to_relative(place_ref, spread, rows, sums[1] / count, 4)
        valid = valid_ref[...]
        for row in range(blocks):
            lanes = slice(row * LANES, (row + 1) * LANES)
            one = lambda slot: rows[slot, row : row + 1, :]
            zhat = (columns_of(z_refs, row) - one(0)) * one(1)
            value = one(2) * (grad_ref[:, lanes] - valid * (one(4) + zhat * one(3)))
            out_ref[:, lanes] = value
            if (row // per) % 2:
                at = (row // per // 2) * width + (row % per) * LANES
                leave_ref[:, at : at + LANES] = value
            high, low = split(value)
            inner = slice((row % per) * LANES, (row % per + 1) * LANES)
            high_s[row // per, :, inner] = high
            low_s[row // per, :, inner] = low

    value = input_terms(high_s, low_s, weight_blocks(place_ref, weights, far_ref))
    for step, (term_ref, first) in enumerate(zip(term_refs, starts)):

        @pl.when(pl.program_id(0) == step)
        def _():
            for pair in range(2):
                at = pl.multiple_of(((place_ref[0] & 1) ^ pair) * width, width)
                term_ref[:, pl.ds(first + at, width)] = value[
                    :, pair * width : (pair + 1) * width
                ]


def norm_back(columns, place, grad, z, params, valid, stats, sums, weights, layer, split_terms):
    frames, features = grad.shape
    width = features // 4
    blocks = features // LANES
    whole = lambda array: pl.BlockSpec(array.shape, lambda s, cols, place: (0,) * array.ndim)
    operands = [grad, *[in_hbm(a) for a in z], params, valid, stats, sums]
    full = jax.ShapeDtypeStruct((frames, features), F32)
    half = jax.ShapeDtypeStruct((frames, 2 * width), F32)
    terms = [half, half] if split_terms else [full]
    out_shape = [full, half, *terms, jax.ShapeDtypeStruct((3, blocks, LANES), F32)]
    return call(
        partial(norm_back_body, len(z), split_terms, layer),
        grid_spec=pltpu.PrefetchScalarGridSpec(
            num_scalar_prefetch=2,
            grid=(2,),
            in_specs=[whole(a) for a in operands] + weight_specs(weights, layer),
            out_specs=[whole(a) for a in out_shape],
            scratch_shapes=[
                pltpu.VMEM((5, blocks, LANES), F32),
                pltpu.VMEM((blocks, LANES), F32),
                pltpu.VMEM((4, frames, width), BF16),
                pltpu.VMEM((4, frames, width), BF16),
                far_scratch(width),
            ],
        ),
        out_shape=out_shape,
        hbm_outs=(0,),
        cost_estimate=cost(6 * frames * features * features, 4 * features * features),
        name="norm_back",
    )(columns, place, *operands, *[in_hbm(w) for w in weights])


def own_terms_body(n_ups, spots, cols_ref, place_ref, grad_ref, *refs):
    del cols_ref
    ups, refs = refs[:n_ups], refs[n_ups:]
    weights, refs = refs[:10], refs[10:]
    out_ref, high_s, low_s, far_ref = refs
    width = high_s.shape[2]
    step = pl.program_id(0)

    @pl.when(step == 0)
    def _():
        for block in range(4):
            high, low = split(grad_ref[:, block * width : (block + 1) * width])
            high_s[block] = high
            low_s[block] = low

    value = input_terms(high_s, low_s, weight_blocks(place_ref, weights, far_ref))
    for pair in range(2):
        at = pl.multiple_of(((place_ref[0] & 1) ^ pair) * width, width)
        out_ref[:, pl.ds(at, width)] = value[:, pair * width : (pair + 1) * width]
    for half in range(2):

        @pl.when(step == half)
        def _():
            first = 2 * half * width
            for (_, column), up in zip(spots, ups):
                low = max(column, first)
                high = min(column + up.shape[1], first + 2 * width)
                if low < high:
                    out_ref[:, low - first : high - first] += up[:, low - column : high - column]


def own_terms(columns, place, grad, ups, weights, layer):
    frames, features = grad.shape
    width = features // 4
    whole = lambda array: pl.BlockSpec(array.shape, lambda s, cols, place: (0,) * array.ndim)
    step_block = pl.BlockSpec((frames, 2 * width), lambda s, cols, place: (0, s))
    return call(
        partial(own_terms_body, len(ups), spots_of_sum(ups, width)),
        grid_spec=pltpu.PrefetchScalarGridSpec(
            num_scalar_prefetch=2,
            grid=(2,),
            in_specs=[whole(grad)]
            + [part_spec(up, frames) for up in ups]
            + weight_specs(weights, layer),
            out_specs=step_block,
            scratch_shapes=[pltpu.VMEM((4, frames, width), BF16)] * 2 + [far_scratch(width)],
        ),
        out_shape=jax.ShapeDtypeStruct((frames, features), F32),
        cost_estimate=cost(6 * frames * features * features, 4 * features * features),
        name="own_terms",
    )(columns, place, in_hbm(grad), *arrays_of(ups), *[in_hbm(w) for w in weights])


def prepare_body(lists_ref, place_ref, own_ref, near_ref, high_ref, low_ref):
    del lists_ref
    padded = high_ref.shape[0] // 2
    width = high_ref.shape[1] // 2
    for clip, part in enumerate((own_ref, near_ref)):
        rows = part.shape[0]
        for dc in range(2):
            at = pl.multiple_of((place_ref[6] ^ clip ^ dc) * width, width)
            high, low = split(part[:, dc * width : (dc + 1) * width])
            high_ref[clip * padded : clip * padded + rows, pl.ds(at, width)] = high
            low_ref[clip * padded : clip * padded + rows, pl.ds(at, width)] = low
        zeros = jnp.zeros((padded - rows, 2 * width), BF16)
        high_ref[clip * padded + rows : (clip + 1) * padded, :] = zeros
        low_ref[clip * padded + rows : (clip + 1) * padded, :] = zeros


def prepare(place, own, near):
    frames, features = own.shape
    width = features // 4
    padded = -(-frames // LANES) * LANES
    in_spec = pl.BlockSpec((frames, 2 * width), lambda s, *_: (0, s))
    out = jax.ShapeDtypeStruct((2 * padded, features), BF16)
    out_spec = pl.BlockSpec((2 * padded, 2 * width), lambda s, order, place: (0, order[s]))
    order = jnp.stack([place[0] >> 1, 1 - (place[0] >> 1)])
    return call(
        prepare_body,
        grid_spec=pltpu.PrefetchScalarGridSpec(
            num_scalar_prefetch=2,
            grid=(2,),
            in_specs=[in_spec, in_spec],
            out_specs=[out_spec, out_spec],
        ),
        out_shape=[out, out],
        hbm_outs=(0, 1),
        cost_estimate=cost(0, 16 * frames * features),
        name="prepare",
    )(order, place, in_hbm(own), in_hbm(near))


def product(g_high, g_low, x_high, x_low):
    return dot(g_high, x_high, NN) + (dot(g_high, x_low, NN) + dot(g_low, x_high, NN))


def weight_body(turn, place_ref, *refs):
    if turn:
        grad_ref, near_ref, x_high, x_low, kept, sent, g_high, g_low, t_high, t_low = refs

        @pl.when(pl.program_id(0) == 0)
        def _():
            frames, features = grad_ref.shape
            width = features // 4
            rows = width // 4
            padded = t_high.shape[1] // 2
            t_high[...] = jnp.zeros_like(t_high)
            t_low[...] = jnp.zeros_like(t_low)
            for clip in range(2):
                for dh in range(2):
                    if clip == 0:
                        part = grad_ref[:, 2 * dh * width : (2 * dh + 1) * width]
                    else:
                        part = near_ref[:, dh * width : (dh + 1) * width]
                    high, low = split(part.T)
                    at = (
                        slice(dh * width, (dh + 1) * width),
                        slice(clip * padded, clip * padded + frames),
                    )
                    t_high[at] = high
                    t_low[at] = low
            for group in range(8):
                first, second, dh = group // 4, group // 2 % 2, group % 2
                core = place_ref[6]
                y = place_ref[4] ^ (first * core + second * (1 - core))
                x = place_ref[5] ^ (first * (1 - core) + second * core)
                at = pl.multiple_of(dh * width + (2 * y + x) * rows, rows)
                g_high[group * rows : (group + 1) * rows, :] = t_high[pl.ds(at, rows), :]
                g_low[group * rows : (group + 1) * rows, :] = t_low[pl.ds(at, rows), :]

    else:
        g_high, g_low, x_high, x_low, kept, sent = refs
    half = g_high.shape[0] // 2
    value = product(g_high[...], g_low[...], x_high[...], x_low[...])
    kept[...] = value[:half].reshape(kept.shape)
    sent[...] = value[half:].reshape(sent.shape)


def weight_rows(side, place, grads, x_split, width):
    turn = side == 0
    whole = lambda array: pl.BlockSpec(array.shape, lambda s, place: (0,) * array.ndim)
    x_spec = pl.BlockSpec((x_split[0].shape[0], width), lambda s, place: (0, s))
    shape = (2, 2, width // 4, 4 * width)
    out_shape = [jax.ShapeDtypeStruct(shape, F32)] * 2
    out_specs = [pl.BlockSpec(shape[:3] + (width,), lambda s, place: (0, 0, 0, s))] * 2
    scratch = []
    if turn:
        turned = (2 * width, x_split[0].shape[0])
        out_shape += [jax.ShapeDtypeStruct(turned, BF16)] * 2
        out_specs += [whole(out_shape[-1])] * 2
        scratch = [pltpu.VMEM(turned, BF16)] * 2
    return call(
        partial(weight_body, turn),
        grid_spec=pltpu.PrefetchScalarGridSpec(
            num_scalar_prefetch=1,
            grid=(4,),
            in_specs=[whole(a) for a in grads] + [x_spec] * 2,
            out_specs=out_specs,
            scratch_shapes=scratch,
        ),
        out_shape=out_shape,
        hbm_outs=(0,),
        cost_estimate=cost(12 * x_split[0].shape[0] * width * 4 * width, 4 * 8 * width * width),
        name="weight_rows",
    )(place, *([in_hbm(grads[0]), grads[1]] if turn else grads), *[in_hbm(x) for x in x_split])


def step_body(n, widths, cut, *refs):
    ins, outs = refs[: 2 * n], refs[2 * n :]
    starts = [sum(widths[:i]) for i in range(len(widths))]
    column = 0
    for i in range(n):
        total = ins[2 * i][...] + ins[2 * i + 1][...]
        end = column + total.shape[-1]
        for j, (start, columns) in enumerate(zip(starts, widths)):
            low, high = max(start, column), min(start + columns, end)
            if low < high:
                to = (Ellipsis, slice(low - start, high - start))
                piece = total[..., low - column : high - column]
                pieces = [piece]
                for _ in range(cut):
                    pieces = [half[k] for half in pieces for k in range(2)]
                for k, some in enumerate(pieces):
                    outs[len(pieces) * j + k][to] = some
        column = end


def step_of(*pairs, cut=1, widths=None):
    shape = list(pairs[0][0].shape)
    widths = widths or [sum(pair[0].shape[-1] for pair in pairs)]
    outs = []
    for columns in widths:
        shape[-1] = columns
        outs += [jax.ShapeDtypeStruct(tuple(shape[cut:]), F32)] * 2**cut
    whole = lambda array: pl.BlockSpec(array.shape, lambda i: (0,) * array.ndim)
    operands = [array for pair in pairs for array in pair]
    return call(
        partial(step_body, len(pairs), widths, cut),
        grid=(1,),
        in_specs=[whole(a) for a in operands],
        out_specs=[whole(a) for a in outs],
        out_shape=outs,
        cost_estimate=cost(0, 4 * sum(a.size for a in operands)),
        name="reduction_step",
    )(*operands)


def plane_swap(array, step):
    pairs = []
    for i in range(8):
        over_x = (i % 2 == 0) == (step == 0)
        pairs.append((i, i ^ 2 if over_x else i ^ 4))
    return lax.ppermute(array, ("y", "x", "c"), pairs)


def plane_gather(share, *before):
    first = plane_swap(share, 0)
    second = plane_swap(share, 1)
    return [share, second, first, plane_swap(after(first, second, *before), 1)]


def assemble_body(place_ref, *refs):
    out_ref = refs[-1]
    core = place_ref[6]
    rows, columns = refs[0].shape
    quarter = columns // 4
    for i in range(4):
        first, second = i // 2, i % 2
        y = place_ref[4] ^ (first * core + second * (1 - core))
        x = place_ref[5] ^ (first * (1 - core) + second * core)
        at = pl.multiple_of((2 * y + x) * rows, rows)
        for side in range(2):
            for h in range(2):
                to = pl.multiple_of((2 * h + (place_ref[7] ^ side)) * quarter, quarter)
                some = slice((2 * side + h) * quarter, (2 * side + h + 1) * quarter)
                out_ref[0, pl.ds(at, rows), pl.ds(to, quarter)] = refs[i][:, some]


def assemble(place, pieces, layer, onto=None):
    rows, columns = 4 * pieces[0].shape[0], pieces[0].shape[1]
    aliases, extra, extra_specs = {}, [], []
    if onto is not None:
        aliases, extra = {1 + len(pieces): 0}, [onto]
        extra_specs = [pl.BlockSpec(memory_space=pl.ANY)]
    (out,) = call(
        assemble_body,
        grid=(1,),
        out_shape=[jax.ShapeDtypeStruct((LAYERS, rows, columns), F32)],
        hbm_outs=(0,),
        in_specs=[SMEM_SPEC]
        + [pl.BlockSpec(p.shape, lambda i: (0, 0)) for p in pieces]
        + extra_specs,
        out_specs=[pl.BlockSpec((1, rows, columns), lambda i: (layer, 0, 0))],
        input_output_aliases=aliases,
        cost_estimate=cost(0, 8 * rows * columns),
        name="assemble",
    )(place, *[p if extra else in_hbm(p) for p in pieces], *extra)
    return out


def half_features(inputs, weights, gains, shifts, decays, biases, lengths, frame_mask, grad_out):
    width, slots = inputs.shape
    clips, frames = frame_mask.shape
    depth = weights.shape[2]
    blocks = 4 * width // LANES
    y, x, h, l, c = (lax.axis_index(name) for name in ("y", "x", "h", "l", "c"))
    b = 2 * y + x
    numbers = [2 * (h ^ (rel // 2)) + (c ^ (rel % 2)) for rel in range(4)] + [y, x, c, l]
    place = jnp.stack(numbers).astype(jnp.int32)
    own_blocks, other_blocks = (
        jnp.stack(
            [2 * (2 * (h ^ (rel // 2)) + half) + (c ^ (rel % 2)) for rel in range(4)]
        ).astype(jnp.int32)
        for half in (l, 1 - l)
    )
    own_columns = jnp.stack([2 * h + l, 2 * (1 - h) + l]).astype(jnp.int32)
    other_columns = jnp.stack([2 * (1 - h) + 1 - l, 2 * h + 1 - l]).astype(jnp.int32)
    rows = width // 4

    clip = 2 * h + c
    seen = lax.dynamic_index_in_dim(frame_mask, clip, 0, keepdims=False)
    length = lax.dynamic_index_in_dim(lengths, clip, 0, keepdims=False)
    moments = jnp.arange(frames, dtype=jnp.int32)
    gate = ((moments < length) & ((seen == 1) | (moments == 0))).astype(F32)
    valid = jnp.broadcast_to(gate[:, None], (frames, LANES))

    def far_share(layer):
        return lax.dynamic_slice(weights, (layer, b * rows, 0), (1, rows, depth))[0]

    def over_h(array):
        return lax.ppermute(array, "h", FLIP2)

    def over_c(array):
        return lax.ppermute(array, "c", FLIP2)

    def over_second(array):
        return plane_swap(array, 1)

    def four_of(near_rows, far_rows):
        return [
            (near_rows, 0),
            (over_c(near_rows), 1),
            (far_rows, 0),
            (over_c(far_rows), 1),
        ]

    def four_of_plane(share):
        both = lax.ppermute(share, ("y", "x"), DIAGONAL)
        return [share, lax.ppermute(share, "x", FLIP2), lax.ppermute(share, "y", FLIP2), both]

    near = over_c(weights)
    share = far_share(0)
    close, away = pack(place, after(inputs, share), frames)
    share = over_h(share)
    away = over_h(away)
    other_close = swap_half(close)
    up_close, up_away = pack(place, after(grad_out, close), frames, waits=True)
    share = after(share, up_close, valid, near, other_close)
    pieces = four_of_plane(share)
    away = after(away, pieces[1:])
    half_weights = [[weights, near, *pieces, *map(over_c, after(pieces, away))]]
    own = four_of(after(close, away), away)
    other_away = swap_half(away)
    others = [(other_close, 0), (over_c(other_close), 1)]
    params = jnp.stack([gains, shifts + biases, decays], axis=1)
    own_params = params.reshape(LAYERS * 3 * width // LANES, LANES)
    params = None

    def gather(array, axes):
        return lax.all_gather(array, axes, tiled=True)

    weight = half_weights[0]
    early = jnp.concatenate([own_blocks, other_blocks[:2]])
    z, own_flat = project(place, frames, own + others, early, weight, 0, flat=own)
    others += [(other_away, 0), (over_c(after(other_away, z)), 1)]
    share = lax.ppermute(after(far_share(1), z), ("h", "c"), DIAGONAL)
    z, stats, other_flat = project(
        place,
        frames,
        others[2:],
        other_blocks[2:],
        weight,
        0,
        z,
        valid,
        params=own_params,
        flat=others,
    )
    z = [z]
    stats = gather(stats, ("y", "x"))
    stats = gather(after(stats, share), ("h", "c"))
    x, states, slopes, params = recur(0, place, gate, z, stats, None, valid, own_flat, False)
    own_near, other_near = over_c(after(own_flat, slopes)), over_c(after(other_flat, slopes))
    x_near = over_c(x)
    own_split = prepare(place, after(own_flat, x_near), own_near)
    other_split = prepare(place, after(other_flat, x_near), other_near)
    saved = [(own_split, other_split, z, stats, states, slopes)]

    pieces = four_of_plane(over_c(after(share, stats)))
    other = swap_half(x)
    own_split = prepare(place, after(x, own_split[0], other_split[0]), x_near)
    half_weights.append([weights, near, *pieces, *map(over_c, after(pieces, own_split[0]))])
    x_own = after(x, own_split[0])
    z, *_ = project(place, frames, [(x_own, None)], own_blocks, half_weights[1], 1)
    up_away = over_h(after(up_away, other, z))
    z, stats = project(
        place, frames, [(other, None)], other_blocks, half_weights[1], 1, z, valid
    )
    z = [z]
    stats = gather(gather(stats, ("y", "x")), ("h", "c"))
    upstream = four_of(up_close, after(up_away, stats))
    *output, states, slopes = recur(1, place, gate, z, stats, params, valid, x, True)
    other_near = over_c(after(other, slopes))
    saved.append((own_split, (other, other_near), z, stats, states, slopes))
    diagonal = over_c(over_h(output[3]))

    ups = upstream
    results = [None] * LAYERS
    for layer in range(LAYERS - 1, -1, -1):
        own_split, other_split, z, stats, states, slopes = saved[layer]
        weight = half_weights[layer]
        grad_pre, sums = back(layer, place, gate, z, stats, params, ups, states, slopes)
        sums = gather(sums, ("y", "x"))
        if layer == 0:
            come[0] = after(come[0], sums, away, output[1][0])
            later, go = step_of((in_hbm(stay[0]), come[0]), (in_hbm(stay[1]), come[1]))
            sums = after(sums, later)
            go = over_second(go)
        sums = gather(sums, ("h", "c"))
        grad_z, leaving, *terms, sums = norm_back(
            other_columns, place, grad_pre, z, params, valid, stats, sums, weight, layer,
            layer == 0,
        )
        leaving = over_c(leaving)
        if layer > 0:
            received = [swap_half(terms[0])]
            other_split = prepare(place, *after(other_split, grad_z))
            leaving = after(leaving, diagonal, other_split[0])
        else:
            received = [None, swap_half(terms[1])]
            later, go = step_of((later, after(go, grad_z)))
            leaving = after(leaving, later)
            go = lax.ppermute(go, ("h", "c"), DIAGONAL)
            later = (later, go)
        *first, g_high, g_low = weight_rows(0, place, (grad_z, leaving), own_split, width)
        turned = (g_high, g_low)
        come = [plane_swap(first[1], 0)]
        if layer == 0:
            received[0] = swap_half(after(terms[0], received[1]))
        second = weight_rows(1, place, turned, other_split, width)
        come.append(plane_swap(second[1], 0))
        stay = (first[0], second[0])
        kept = own_terms(own_columns, place, after(grad_z, second[0]), ups, weight, layer)
        if layer > 0:
            away = over_h(after(output[2], kept))
            output = [(a, 0) for a in (output[0], over_c(output[1]), away, diagonal)]
        ups = [(kept, None)] + [(r, None) for r in received]
        results[layer] = lax.dynamic_index_in_dim(
            sums.reshape(3, 4, width), clip, axis=1, keepdims=False
        )

    sums = jnp.stack(results)
    sums = [sums[:, 0], sums[:, 1], sums[:, 2]]
    aways = merge(kept, 1, received[1], apart=True)
    later = (later[0], over_c(after(later[1], aways[0])))
    come[0] = after(come[0], sums, later[1])
    far_near = over_c(lax.ppermute(aways[0], ("h", "c"), DIAGONAL))
    near_sum, far_sum, near_go, far_go = step_of(
        (in_hbm(stay[0]), come[0]), (in_hbm(stay[1]), come[1]), cut=2
    )
    near_go, far_go = over_second(near_go), over_second(far_go)
    (go,) = step_of((far_sum, after(far_go, far_near)), cut=0)
    (later,) = step_of(later, cut=0)
    later = after(later, go)
    go = over_h(go)
    later = plane_gather(later)
    (total,) = step_of((near_sum, near_go), cut=0)
    output = unpack(place, [(after(array, total), i) for array, i in output], frames, waited=True)
    close = merge(kept, 0, after(received[0], output))
    far = over_c(over_h(after(aways[1], go)))
    (share,) = step_of((total, after(go, close, *later[1:])), cut=0)
    grad_weights = assemble(place, after(later, share), 1)
    gathered = plane_gather(share, grad_weights)
    grad_in = [(close, 0), (over_c(close[frames:]), 0), (far_near, 0), (far, 0)]
    grad_in = unpack(place, grad_in, frames)
    grad_weights = assemble(place, after(gathered, grad_in), 0, grad_weights)
    return (output, grad_in, grad_weights, *sums, sums[1])


def gelu_slope(value):
    return (
        0.5 * (1.0 + jax.scipy.special.erf(value / ROOT_TWO))
        + value * jnp.exp(-0.5 * value * value) / ROOT_TWO_PI
    )


def recur_step(decay, state, inputs):
    drive_t, valid_t = inputs
    pre = drive_t + decay * state
    state = state + valid_t * (jax.nn.gelu(pre, approximate=False) - state)
    return (state, state)


def back_step(decay, carry, inputs):
    upstream_t, valid_t, pre_t = inputs
    total = upstream_t + carry
    grad_pre = total * valid_t * gelu_slope(pre_t)
    carry = total * (1.0 - valid_t) + grad_pre * decay
    return (carry, grad_pre)


def add_piece(weight, piece):
    return jnp.dot(weight, piece, precision=HIGH, preferred_element_type=jnp.float32)


def weight_columns(grad_pre_norm, piece):
    return jnp.einsum("jf,kf->jk", grad_pre_norm, piece, precision=HIGH)


def split_features(inputs, weights, gains, shifts, decays, biases, lengths, frame_mask, grad_out):
    width, slots = inputs.shape
    clips, frames_len = frame_mask.shape
    frames = jnp.arange(frames_len, dtype=jnp.int32)
    valid_grid = (
        (frames[None, :] < lengths[:, None]) & ((frame_mask == 1) | (frames[None, :] == 0))
    ).astype(jnp.float32)
    valid = valid_grid.reshape(-1)
    valid_row = valid[None, :]
    valid_time = jnp.broadcast_to(valid_grid.T[:, :, None], (frames_len, clips, width)).reshape(
        frames_len, clips * width
    )
    count_local = jnp.sum(valid)

    def to_time(array):
        return jnp.transpose(array.reshape(width, clips, frames_len), (2, 1, 0)).reshape(
            frames_len, clips * width
        )

    def from_time(array):
        return jnp.transpose(array.reshape(frames_len, clips, width), (2, 1, 0)).reshape(
            width, slots
        )

    layer_in = inputs
    saved = []
    for layer_no in range(LAYERS):
        weight = weights[layer_no]
        gathered = lax.all_gather(layer_in, "neuron", axis=0, tiled=True)
        pre_norm = add_piece(weight, gathered)
        first_sum, count = lax.psum((jnp.sum(valid_row * pre_norm, axis=1), count_local), "batch")
        mean = first_sum / count
        centered = pre_norm - mean[:, None]
        var = lax.psum(jnp.sum(valid_row * centered * centered, axis=1), "batch") / count
        inv_std = lax.rsqrt(var + EPS)
        zhat = (pre_norm - mean[:, None]) * inv_std[:, None]
        drive = gains[layer_no][:, None] * zhat + (shifts[layer_no] + biases[layer_no])[:, None]
        drive_time = to_time(drive)
        decay_wide = jnp.tile(decays[layer_no], clips)
        start_state = jnp.zeros((clips * width,), jnp.float32)
        _, states = lax.scan(
            partial(recur_step, decay_wide), start_state, (drive_time, valid_time), unroll=8
        )
        saved.append((gathered, zhat, inv_std, drive_time, states, count))
        layer_in = layer_in + valid_row * from_time(states)
    upstream = grad_out
    grad_parts = [None] * LAYERS
    for layer_no in range(LAYERS - 1, -1, -1):
        gathered, zhat, inv_std, drive_time, states, count = saved[layer_no]
        decay_wide = jnp.tile(decays[layer_no], clips)
        gain = gains[layer_no]
        previous = jnp.concatenate([jnp.zeros_like(states[:1]), states[:-1]], axis=0)
        pre_time = drive_time + decay_wide[None, :] * previous
        grad_state = to_time(valid_row * upstream)
        start_carry = jnp.zeros((clips * width,), jnp.float32)
        _, grad_pre_time = lax.scan(
            partial(back_step, decay_wide),
            start_carry,
            (grad_state, valid_time, pre_time),
            reverse=True,
            unroll=8,
        )
        decay_local = jnp.sum(
            jnp.sum(grad_pre_time * previous, axis=0).reshape(clips, width), axis=0
        )
        grad_pre = from_time(grad_pre_time)
        gain_local = jnp.sum(grad_pre * zhat, axis=1)
        shift_local = jnp.sum(grad_pre, axis=1)
        grad_gain, grad_shift, grad_decay = lax.psum(
            (gain_local, shift_local, decay_local), "batch"
        )
        grad_pre_norm = (gain * inv_std)[:, None] * (
            grad_pre - valid_row * (grad_shift[:, None] + zhat * grad_gain[:, None]) / count
        )
        weight_local = weight_columns(grad_pre_norm, gathered)
        input_terms = jnp.einsum("jk,jf->kf", weights[layer_no], grad_pre_norm, precision=HIGH)
        input_grad = lax.psum_scatter(input_terms, "neuron", scatter_dimension=0, tiled=True)
        grad_weight = lax.psum(weight_local, "batch")
        upstream = upstream + input_grad
        grad_parts[layer_no] = (grad_weight, grad_gain, grad_shift, grad_decay)
    grad_weights = jnp.stack([grad_parts[layer_no][0] for layer_no in range(LAYERS)])
    grad_gains = jnp.stack([grad_parts[layer_no][1] for layer_no in range(LAYERS)])
    grad_shifts = jnp.stack([grad_parts[layer_no][2] for layer_no in range(LAYERS)])
    grad_decays = jnp.stack([grad_parts[layer_no][3] for layer_no in range(LAYERS)])
    return (layer_in, upstream, grad_weights, grad_gains, grad_shifts, grad_decays, grad_shifts)


def solution(mesh):
    if (mesh.shape["batch"], mesh.shape["neuron"]) == (4, 8):
        cut = Mesh(mesh.devices.reshape(2, 2, 2, 2, 2), ("y", "x", "h", "l", "c"))
        batch, neuron, body = ("y", "x"), ("h", "l", "c"), half_features
    else:
        cut, batch, neuron, body = mesh, "batch", "neuron", split_features
    in_specs = (
        P(neuron, batch),
        P(None, neuron, None),
        P(None, neuron),
        P(None, neuron),
        P(None, neuron),
        P(None, neuron),
        P(batch),
        P(batch, None),
        P(neuron, batch),
    )
    out_specs = (
        P(neuron, batch),
        P(neuron, batch),
        P(None, neuron, None),
        P(None, neuron),
        P(None, neuron),
        P(None, neuron),
        P(None, neuron),
    )
    return jax.shard_map(
        body, mesh=cut, in_specs=in_specs, out_specs=out_specs, check_vma=False
    )
```

```python
from functools import partial
import math

import jax
import jax.numpy as jnp
from jax import lax
from jax.experimental import pallas as pl
from jax.experimental.pallas import tpu as pltpu
from jax.sharding import Mesh, PartitionSpec as P

LAYERS = 2
EPS = 1e-05
HIGH = lax.Precision.HIGHEST
ROOT_TWO = math.sqrt(2.0)
ROOT_TWO_PI = math.sqrt(2.0 * math.pi)
F32 = jnp.float32
BF16 = jnp.bfloat16
LANES = 128
VMEM_LIMIT = 24 * 1024 * 1024
SMEM_SPEC = pl.BlockSpec(memory_space=pltpu.SMEM)
VMEM_SPEC = pl.BlockSpec(memory_space=pltpu.VMEM)


FLIP2 = [(0, 1), (1, 0)]
DIAGONAL = [(0, 3), (1, 2), (2, 1), (3, 0)]


def swap_half(array):
    return lax.ppermute(array, "l", FLIP2)


def after(value, *others):
    return lax.optimization_barrier((value, others))[0]


def split(value):
    high = value.astype(BF16)
    return high, (value - high.astype(F32)).astype(BF16)


def dot(a, b, dims):
    return lax.dot_general(a, b, (dims, ((), ())), preferred_element_type=F32)


NT = ((1,), (1,))
NN = ((1,), (0,))


def in_hbm(array):
    return pltpu.with_memory_space_constraint(array, pltpu.HBM)


def call(body, out_shape, hbm_outs=(), **kwargs):
    if hbm_outs:
        out_shape = [
            pltpu.HBM(a.shape, a.dtype) if i in hbm_outs else a for i, a in enumerate(out_shape)
        ]
    return pl.pallas_call(
        body,
        out_shape=out_shape,
        compiler_params=pltpu.CompilerParams(vmem_limit_bytes=VMEM_LIMIT),
        **kwargs,
    )


def cost(flops, byte_count):
    return pl.CostEstimate(flops=int(flops) // 64, bytes_accessed=int(byte_count) // 64, transcendentals=0)


def pack_body(frames, place_ref, in_ref, near_ref, far_ref, turned):
    slots = in_ref.shape[1]
    for start in range(0, slots, LANES):
        turned[start : start + LANES, :] = in_ref[:, start : start + LANES].T
    for rel in range(4):
        first = pl.multiple_of(place_ref[rel] * frames, 8)
        out = (near_ref, far_ref)[rel // 2]
        out[(rel % 2) * frames : (rel % 2 + 1) * frames, :] = turned[pl.ds(first, frames), :]


def pack(place, array, frames, waits=False):
    width, slots = array.shape
    out = jax.ShapeDtypeStruct((2 * frames, width), F32)
    return call(
        partial(pack_body, frames),
        grid=(1,),
        out_shape=[out, out],
        in_specs=[SMEM_SPEC, pl.BlockSpec((width, slots), lambda i: (0, 0))],
        out_specs=[pl.BlockSpec(out.shape, lambda i: (0, 0))] * 2,
        scratch_shapes=[pltpu.VMEM((slots, width), F32)],
        hbm_outs=(0, 1) if waits else (),
        cost_estimate=cost(0, 8 * width * slots),
        name="pack",
    )(place, in_hbm(array))


def part_spec(part, frames):
    array, i = part
    if i is None:
        return pl.BlockSpec(array.shape, lambda *_: (0,) * array.ndim)
    return pl.BlockSpec((frames, array.shape[1]), lambda *_: (i, 0))


def arrays_of(parts):
    return [array for array, _ in parts]


def unpack_body(frames, place_ref, *refs):
    ins, out_ref, turned = refs[:4], refs[4], refs[5]
    slots = out_ref.shape[1]
    for rel in range(4):
        first = pl.multiple_of(place_ref[rel] * frames, 8)
        turned[pl.ds(first, frames), :] = ins[rel][...]
    for start in range(0, slots, LANES):
        out_ref[:, start : start + LANES] = turned[start : start + LANES, :].T


def unpack(place, parts, frames, waited=False):
    width = parts[0][0].shape[1]
    slots = 4 * frames
    return call(
        partial(unpack_body, frames),
        grid=(1,),
        out_shape=jax.ShapeDtypeStruct((width, slots), F32),
        in_specs=[SMEM_SPEC] + [part_spec(part, frames) for part in parts],
        out_specs=pl.BlockSpec((width, slots), lambda i: (0, 0)),
        scratch_shapes=[pltpu.VMEM((slots, width), F32)],
        cost_estimate=cost(0, 8 * width * slots),
        name="unpack",
    )(place, *[in_hbm(a) if waited else a for a in arrays_of(parts)])


def merge_body(kept_ref, come_ref, *outs):
    frames, columns = kept_ref.shape
    width = columns // 2
    for i in range(2):
        some = slice(i * width, (i + 1) * width)
        if len(outs) > 1:
            outs[i][...] = kept_ref[:, some] + come_ref[:, some]
            continue
        (out_ref,) = outs
        out_ref[i * frames : (i + 1) * frames, :] = kept_ref[:, some] + come_ref[:, some]


def merge(kept, half, come, apart=False):
    frames, columns = come.shape
    rows, n = (frames, 2) if apart else (2 * frames, 1)
    outs = call(
        merge_body,
        hbm_outs=(0, 1) if apart else (),
        grid=(1,),
        out_shape=[jax.ShapeDtypeStruct((rows, columns // 2), F32)] * n,
        in_specs=[
            pl.BlockSpec((frames, columns), lambda i: (0, half)),
            pl.BlockSpec((frames, columns), lambda i: (0, 0)),
        ],
        out_specs=[pl.BlockSpec((rows, columns // 2), lambda i: (0, 0))] * n,
        cost_estimate=cost(0, 12 * frames * columns),
        name="merge",
    )(kept, come)
    return outs if apart else outs[0]


def project_body(n_parts, n_flat, spots, n_weights, first, with_acc, with_stats, with_params, cols_ref, place_ref, *refs):
    del cols_ref

    def take(n):
        nonlocal refs
        some, refs = refs[:n], refs[n:]
        return some

    parts, flat_parts, weights = take(n_parts), take(n_flat), take(n_weights)
    acc, valid, stats_in, params = take(with_acc), take(with_stats > 0), take(with_stats > 1), take(with_params)
    (out_ref,) = take(1)
    stats, flat = take(with_stats > 0), take(n_flat > 0)
    x_high, x_low, far_ref = refs
    step = pl.program_id(0)
    width = x_high.shape[2]

    @pl.when(step == 0)
    def _():
        for block, part in zip(spots, parts):
            for start in range(0, part.shape[1], width):
                high, low = split(part[:, start : start + width])
                x_high[block + start // width] = high
                x_low[block + start // width] = low
        column = 0
        for part in flat_parts:
            flat[0][:, column : column + part.shape[1]] = part[...]
            column += part.shape[1]
        if with_acc:
            out_ref[...] = acc[0][...]
        else:
            out_ref[...] = jnp.zeros_like(out_ref)

    stacked = jnp.concatenate([x_high[step], x_low[step], x_high[step]], axis=1)
    for block, weight in enumerate(weight_blocks(place_ref, weights, far_ref)):
        w_high, w_low = split(weight)
        columns = slice(block * width, (block + 1) * width)
        out_ref[:, columns] += dot(stacked, jnp.concatenate([w_high, w_high, w_low], axis=1), NT)

    if with_stats:
        (stats_ref,) = stats

        @pl.when(step == pl.num_programs(0) - 1)
        def _():
            if stats_in:
                stats_ref[...] = stats_in[0][...]
            own = jnp.sum(valid[0][...], axis=0, keepdims=True)
            per = width // LANES
            for row in range(out_ref.shape[1] // LANES):
                z = out_ref[:, row * LANES : (row + 1) * LANES]
                total = jnp.sum(valid[0][...] * z, axis=0, keepdims=True)
                centred = valid[0][...] * (z - total / own)
                squares = jnp.sum(centred * centred, axis=0, keepdims=True)
                at = place_ref[first + row // per] * per + row % per
                stats_ref[0, pl.ds(at, 1), :] = total
                stats_ref[1, pl.ds(at, 1), :] = squares
                stats_ref[2, pl.ds(at, 1), :] = own
            if with_params:
                rest = params[0].shape[0] - 8
                stats_ref[3] = params[0][:8, :]
                stats_ref[4] = jnp.zeros_like(stats_ref[4])
                stats_ref[4, :rest, :] = params[0][8:, :]


def weight_specs(weights, layer, pairs=2):
    specs = []
    for weight in weights:
        if weight.ndim == 3:
            shape = (1, weight.shape[1], pairs * weight.shape[1])
            specs.append(pl.BlockSpec(shape, lambda s, cols, *_: (layer, 0, cols[s])))
        else:
            shape = (weight.shape[0], pairs * 4 * weight.shape[0])
            specs.append(pl.BlockSpec(shape, lambda s, cols, *_: (0, cols[s])))
    return specs


def far_scratch(width, pairs=2):
    return pltpu.VMEM((2, width, pairs * width), F32)


def weight_blocks(place_ref, refs, far_ref):
    near = [ref[0] for ref in refs if len(ref.shape) == 3]
    pieces = [ref for ref in refs if len(ref.shape) == 2]
    far = []
    for i in range(len(pieces) // 4):
        for rel, piece in enumerate(pieces[4 * i : 4 * i + 4]):
            rows = piece.shape[0]
            row = 2 * (place_ref[4] ^ (rel // 2)) + (place_ref[5] ^ (rel % 2))
            far_ref[i, pl.ds(pl.multiple_of(row * rows, rows), rows), :] = piece[...]
        far.append(far_ref[i])
    return near + far


def project(
    place, frames, parts, blocks, weights, layer, acc=None, valid=None, stats=None, params=None, flat=()
):
    near = weights[0].ndim == 3
    units = sum(1 if w.ndim == 3 else 0.25 for w in weights)
    width = weights[0].shape[1] if near else 4 * weights[0].shape[0]
    n = blocks.shape[0]
    spots, block = [], 0
    for array, _ in parts:
        spots.append(block)
        block += array.shape[1] // width
    full = pl.BlockSpec(memory_space=pltpu.VMEM)
    in_specs = [part_spec(part, frames) for part in (*parts, *flat)]
    in_specs += weight_specs(weights, layer, 1)
    operands = arrays_of(parts) + arrays_of(flat) + [in_hbm(w) for w in weights]
    array = jax.ShapeDtypeStruct((frames, int(units) * width), F32)
    array_spec = pl.BlockSpec(array.shape, lambda s, cols, place: (0, 0))
    out_shape, out_specs = [array], [array_spec]
    if acc is not None:
        in_specs.append(array_spec)
        operands.append(in_hbm(acc))
    if valid is not None:
        in_specs.append(full)
        operands.append(valid)
        shape = (3 if params is None else 5, 4 * width // LANES, LANES)
        out_shape.append(jax.ShapeDtypeStruct(shape, F32))
        out_specs.append(pl.BlockSpec(shape, lambda s, cols, place: (0, 0, 0)))
    for extra in (stats, params):
        if extra is not None:
            in_specs.append(full)
            operands.append(extra)
    if flat:
        out_shape.append(jax.ShapeDtypeStruct((frames, 4 * width), F32))
        out_specs.append(pl.BlockSpec((frames, 4 * width), lambda s, cols, place: (0, 0)))
    return call(
        partial(
            project_body,
            len(parts),
            len(flat),
            spots,
            len(weights),
            0 if near else 2,
            acc is not None,
            (valid is not None) + (stats is not None),
            params is not None,
        ),
        grid_spec=pltpu.PrefetchScalarGridSpec(
            num_scalar_prefetch=2,
            grid=(n,),
            in_specs=in_specs,
            out_specs=out_specs,
            scratch_shapes=[pltpu.VMEM((n, frames, width), BF16)] * 2 + [far_scratch(width, 1)],
        ),
        out_shape=out_shape,
        hbm_outs=(0, len(out_shape) - 1) if flat else (0,),
        cost_estimate=cost(6 * frames * n * width * units * width, 4 * n * width * units * width),
        name="project",
    )(blocks, place, *operands)


def to_relative(place_ref, spread, rows_ref, value, slot):
    per = value.shape[0] // 4
    spread[...] = value
    for rel in range(4):
        first = place_ref[rel] * per
        for row in range(per):
            rows_ref[slot, rel * per + row : rel * per + row + 1, :] = spread[
                pl.ds(first + row, 1), :
            ]


def tree(values):
    while len(values) > 1:
        values = [a + b for a, b in zip(values[::2], values[1::2])]
    return values[0]


def gathered(ref, slot):
    return [ref[i] for i in range(slot, ref.shape[0], ref.shape[0] // 16)]


def norm_terms(stats_ref):
    each = [gathered(stats_ref, slot) for slot in range(3)]
    totals, squares, owns = each
    count = tree(owns)
    mean = tree(totals) / count
    away = [total / own - mean for total, own in zip(totals, owns)]
    spread = tree([s + n * a * a for s, n, a in zip(squares, owns, away)])
    return count, mean, lax.rsqrt(spread / count + EPS)


CHUNKS = 4


def columns_of(refs, row):
    for ref in refs:
        if row * LANES < ref.shape[1]:
            return ref[:, row * LANES : (row + 1) * LANES]
        row -= ref.shape[1] // LANES


def recur_body(n_z, last, layer, spread_params, place_ref, gate_ref, *refs):
    z_refs, refs = refs[:n_z], refs[n_z:]
    (stats_ref, params_ref, valid_ref, x_ref), refs = refs[:4], refs[4:]
    outs, refs = refs[: 1 + 3 * last], refs[1 + 3 * last :]
    if spread_params:
        state_ref, slope_ref, params_out, rows, spread, held, drive_s, state_s, slope_s = refs
    else:
        state_ref, slope_ref, rows, spread, held, drive_s, state_s, slope_s = refs
    frames, features = x_ref.shape
    blocks = features // LANES
    per = blocks // 4
    chunk = pl.program_id(0)

    @pl.when(chunk == 0)
    def _():
        if spread_params:
            for rel in range(4):
                first = place_ref[rel] * (stats_ref.shape[0] // 16) + 3
                for row in range(LAYERS * 3 * per):
                    at = rel * per + row % per
                    params_out[row // per, at : at + 1, :] = stats_ref[
                        first + row // 8, row % 8 : row % 8 + 1, :
                    ]
            params = [params_out[3 * layer + i] for i in range(3)]
        else:
            params = [params_ref[3 * layer + i] for i in range(3)]
        _, mean, inv_std = norm_terms(stats_ref)
        to_relative(place_ref, spread, rows, mean, 0)
        to_relative(place_ref, spread, rows, inv_std, 1)
        rows[1] = rows[1] * params[0]
        rows[2] = params[1]
        rows[3] = params[2]
        held[...] = jnp.zeros_like(held)

    for row in range(blocks):
        drive_s[row * frames : (row + 1) * frames, :] = (
            columns_of(z_refs, row) - rows[0, row : row + 1, :]
        ) * rows[1, row : row + 1, :] + rows[2, row : row + 1, :]
    decay = rows[3]

    def step(t, state):
        at = pl.ds(t, blocks, stride=frames)
        pre = drive_s[at, :] + decay * state
        half = 0.5 + 0.5 * lax.erf(pre * (1.0 / ROOT_TWO))
        gate = gate_ref[chunk * frames + t] > 0.0
        slope = half + pre * jnp.exp(-0.5 * pre * pre) * (1.0 / ROOT_TWO_PI)
        state = jnp.where(gate, pre * half, state)
        state_s[at, :] = state
        slope_s[at, :] = jnp.where(gate, slope, 0.0)
        return state

    held[...] = lax.fori_loop(0, frames, step, held[...], unroll=8)
    valid = valid_ref[...]
    for row in range(blocks):
        lanes = slice(row * LANES, (row + 1) * LANES)
        state = state_s[row * frames : (row + 1) * frames, :]
        state_ref[:, lanes] = state
        slope_ref[:, lanes] = slope_s[row * frames : (row + 1) * frames, :]
        value = x_ref[:, lanes] + valid * state
        out, at = (outs[row // per], row % per) if last else (outs[0], row)
        out[:, at * LANES : (at + 1) * LANES] = value


def recur(layer, place, gate, z, stats, params, valid, x, last):
    frames, features = x.shape
    blocks = features // LANES
    some = frames // CHUNKS
    whole = lambda array: pl.BlockSpec(array.shape, lambda i: (0,) * array.ndim)
    by_chunk = lambda array: pl.BlockSpec((some, array.shape[1]), lambda i: (i, 0))
    full = jax.ShapeDtypeStruct((frames, features), F32)
    piece = jax.ShapeDtypeStruct((frames, features // 4), F32)
    out_shape = [piece] * 4 if last else [full]
    out_shape += [full, full]
    out_specs = [by_chunk(a) for a in out_shape]
    spread_params = params is None
    if spread_params:
        out_shape.append(jax.ShapeDtypeStruct((3 * LAYERS, blocks, LANES), F32))
        out_specs.append(whole(out_shape[-1]))
        params = valid
    return call(
        partial(recur_body, len(z), last, layer, spread_params),
        grid=(CHUNKS,),
        in_specs=[SMEM_SPEC, SMEM_SPEC]
        + [by_chunk(a) for a in z]
        + [whole(a) for a in (stats, params)]
        + [by_chunk(a) for a in (valid, x)],
        out_specs=out_specs,
        out_shape=out_shape,
        hbm_outs=tuple(range(len(out_shape) - spread_params)) if last else (1, 2),
        scratch_shapes=[
            pltpu.VMEM((4, blocks, LANES), F32),
            pltpu.VMEM((blocks, LANES), F32),
            pltpu.VMEM((blocks, LANES), F32),
        ]
        + [pltpu.VMEM((blocks * some, LANES), F32)] * 3,
        cost_estimate=cost(100 * frames * features, 20 * frames * features),
        name="recur",
    )(place, gate, *[in_hbm(a) for a in z], stats, params, valid, in_hbm(x))


def back_body(n_z, n_ups, spots, layer, place_ref, gate_ref, *refs):
    z_refs, refs = refs[:n_z], refs[n_z:]
    (stats_ref, params_ref), refs = refs[:2], refs[2:]
    ups, (state_ref, slope_ref), refs = refs[:n_ups], refs[n_ups : n_ups + 2], refs[n_ups + 2 :]
    grad_ref, sums_ref, rows, spread, held, up_s, state_s, slope_s = refs
    frames, features = state_ref.shape
    blocks = features // LANES
    per = blocks // 4
    tall = frames + 8
    step_no = pl.program_id(0)
    chunk = pl.num_programs(0) - 1 - step_no

    @pl.when(step_no == 0)
    def _():
        _, mean, inv_std = norm_terms(stats_ref)
        to_relative(place_ref, spread, rows, mean, 0)
        to_relative(place_ref, spread, rows, inv_std, 1)
        held[...] = jnp.zeros_like(held)

    for row in range(blocks):
        lanes = slice(row * LANES, (row + 1) * LANES)
        base = row * frames
        up = None
        for (_, column), part in zip(spots, ups):
            if column <= row * LANES < column + part.shape[1]:
                value = part[:, row * LANES - column : (row + 1) * LANES - column]
                up = value if up is None else up + value
        up_s[base : base + frames, :] = up
        state_s[row * tall : row * tall + 8, :] = jnp.zeros((8, LANES), F32)
        state_s[row * tall + 8 : (row + 1) * tall, :] = state_ref[:, lanes]
        slope_s[base : base + frames, :] = slope_ref[:, lanes]
    decay = params_ref[3 * layer + 2]

    def step(i, carry):
        t = frames - 1 - i
        at = pl.ds(t, blocks, stride=frames)
        slope = slope_s[at, :]
        gate = gate_ref[chunk * frames + t]
        total = gate * up_s[at, :] + carry
        up_s[at, :] = total * slope
        return total * (slope * decay + (1.0 - gate))

    held[0] = lax.fori_loop(0, frames, step, held[0], unroll=8)
    held[4] += held[1] * state_s[pl.ds(tall - 1, blocks, stride=tall), :]
    held[1] = up_s[pl.ds(0, blocks, stride=frames), :]
    for row in range(blocks):
        lanes = slice(row * LANES, (row + 1) * LANES)
        grad = up_s[row * frames : (row + 1) * frames, :]
        grad_ref[:, lanes] = grad
        zhat = (columns_of(z_refs, row) - rows[0, row : row + 1, :]) * rows[1, row : row + 1, :]
        before = state_s[row * tall + 7 : row * tall + 7 + frames, :]
        for slot, value in enumerate((grad * zhat, grad, grad * before)):
            held[2 + slot, row : row + 1, :] += jnp.sum(value, axis=0, keepdims=True)

    @pl.when(chunk == 0)
    def _():
        for row in range(blocks):
            at = place_ref[row // per] * per + row % per
            for slot in range(3):
                sums_ref[slot, pl.ds(at, 1), :] = held[2 + slot, row : row + 1, :]


def spots_of_sum(parts, width):
    spots, column = [], 0
    for array, _ in parts:
        spots.append((0, column % (4 * width)))
        column += array.shape[1]
    return spots


def back(layer, place, gate, z, stats, params, ups, states, slopes):
    frames, features = states.shape
    width = features // 4
    blocks = features // LANES
    some = frames // CHUNKS
    whole = lambda array: pl.BlockSpec(array.shape, lambda i: (0,) * array.ndim)

    def by_chunk(array, first=0):
        return pl.BlockSpec(
            (some, array.shape[1]), lambda i: ((first or 0) * CHUNKS + CHUNKS - 1 - i, 0)
        )

    out_shape = [
        jax.ShapeDtypeStruct((frames, features), F32),
        jax.ShapeDtypeStruct((3, blocks, LANES), F32),
    ]
    return call(
        partial(back_body, len(z), len(ups), spots_of_sum(ups, width), layer),
        grid=(CHUNKS,),
        in_specs=[SMEM_SPEC] * 2
        + [by_chunk(a) for a in z]
        + [whole(a) for a in (stats, params)]
        + [by_chunk(*up) for up in ups]
        + [by_chunk(a) for a in (states, slopes)],
        out_specs=[by_chunk(out_shape[0]), whole(out_shape[1])],
        out_shape=out_shape,
        scratch_shapes=[
            pltpu.VMEM((2, blocks, LANES), F32),
            pltpu.VMEM((blocks, LANES), F32),
            pltpu.VMEM((5, blocks, LANES), F32),
            pltpu.VMEM((blocks * some, LANES), F32),
            pltpu.VMEM((blocks * (some + 8), LANES), F32),
            pltpu.VMEM((blocks * some, LANES), F32),
        ],
        cost_estimate=cost(30 * frames * features, 20 * frames * features),
        name="back",
    )(
        place,
        gate,
        *[in_hbm(a) for a in z],
        stats,
        params,
        *arrays_of(ups),
        in_hbm(states),
        in_hbm(slopes),
    )


def input_terms(high_s, low_s, weights):
    left, right = [], []
    for block, weight in enumerate(weights):
        w_high, w_low = split(weight)
        left += [high_s[block], low_s[block], high_s[block]]
        right += [w_high, w_high, w_low]
    return dot(jnp.concatenate(left, axis=1), jnp.concatenate(right, axis=0), NN)


def norm_back_body(n_z, split_terms, layer, cols_ref, place_ref, grad_ref, *refs):
    del cols_ref
    z_refs, refs = refs[:n_z], refs[n_z:]
    params_ref, valid_ref, stats_ref, sums_ref, *refs = refs
    weights, refs = refs[:10], refs[10:]
    if split_terms:
        out_ref, leave_ref, near_term_ref, far_term_ref, sums_out_ref, *refs = refs
        term_refs, starts = (far_term_ref, near_term_ref), (0, 0)
    else:
        out_ref, leave_ref, term_ref, sums_out_ref, *refs = refs
        term_refs, starts = (term_ref, term_ref), (2 * grad_ref.shape[1] // 4, 0)
    rows, spread, high_s, low_s, far_ref = refs
    blocks = grad_ref.shape[1] // LANES
    width = high_s.shape[2]
    per = width // LANES

    @pl.when(pl.program_id(0) == 0)
    def _():
        count, mean, inv_std = norm_terms(stats_ref)
        to_relative(place_ref, spread, rows, mean, 0)
        to_relative(place_ref, spread, rows, inv_std, 1)
        rows[2] = rows[1] * params_ref[3 * layer]
        sums = [tree(gathered(sums_ref, slot)) for slot in range(3)]
        for slot in range(3):
            sums_out_ref[slot] = sums[slot]
        to_relative(place_ref, spread, rows, sums[0] / count, 3)
        to_relative(place_ref, spread, rows, sums[1] / count, 4)
        valid = valid_ref[...]
        for row in range(blocks):
            lanes = slice(row * LANES, (row + 1) * LANES)
            one = lambda slot: rows[slot, row : row + 1, :]
            zhat = (columns_of(z_refs, row) - one(0)) * one(1)
            value = one(2) * (grad_ref[:, lanes] - valid * (one(4) + zhat * one(3)))
            out_ref[:, lanes] = value
            if (row // per) % 2:
                at = (row // per // 2) * width + (row % per) * LANES
                leave_ref[:, at : at + LANES] = value
            high, low = split(value)
            inner = slice((row % per) * LANES, (row % per + 1) * LANES)
            high_s[row // per, :, inner] = high
            low_s[row // per, :, inner] = low

    value = input_terms(high_s, low_s, weight_blocks(place_ref, weights, far_ref))
    for step, (term_ref, first) in enumerate(zip(term_refs, starts)):

        @pl.when(pl.program_id(0) == step)
        def _():
            for pair in range(2):
                at = pl.multiple_of(((place_ref[0] & 1) ^ pair) * width, width)
                term_ref[:, pl.ds(first + at, width)] = value[
                    :, pair * width : (pair + 1) * width
                ]


def norm_back(columns, place, grad, z, params, valid, stats, sums, weights, layer, split_terms):
    frames, features = grad.shape
    width = features // 4
    blocks = features // LANES
    whole = lambda array: pl.BlockSpec(array.shape, lambda s, cols, place: (0,) * array.ndim)
    operands = [grad, *[in_hbm(a) for a in z], params, valid, stats, sums]
    full = jax.ShapeDtypeStruct((frames, features), F32)
    half = jax.ShapeDtypeStruct((frames, 2 * width), F32)
    terms = [half, half] if split_terms else [full]
    out_shape = [full, half, *terms, jax.ShapeDtypeStruct((3, blocks, LANES), F32)]
    return call(
        partial(norm_back_body, len(z), split_terms, layer),
        grid_spec=pltpu.PrefetchScalarGridSpec(
            num_scalar_prefetch=2,
            grid=(2,),
            in_specs=[whole(a) for a in operands] + weight_specs(weights, layer),
            out_specs=[whole(a) for a in out_shape],
            scratch_shapes=[
                pltpu.VMEM((5, blocks, LANES), F32),
                pltpu.VMEM((blocks, LANES), F32),
                pltpu.VMEM((4, frames, width), BF16),
                pltpu.VMEM((4, frames, width), BF16),
                far_scratch(width),
            ],
        ),
        out_shape=out_shape,
        hbm_outs=(0, 2) if split_terms else (0,),
        cost_estimate=cost(6 * frames * features * features, 4 * features * features),
        name="norm_back",
    )(columns, place, *operands, *[in_hbm(w) for w in weights])


def own_terms_body(n_ups, spots, cols_ref, place_ref, grad_ref, *refs):
    del cols_ref
    ups, refs = refs[:n_ups], refs[n_ups:]
    weights, refs = refs[:10], refs[10:]
    out_ref, high_s, low_s, far_ref = refs
    width = high_s.shape[2]
    step = pl.program_id(0)

    @pl.when(step == 0)
    def _():
        for block in range(4):
            high, low = split(grad_ref[:, block * width : (block + 1) * width])
            high_s[block] = high
            low_s[block] = low

    value = input_terms(high_s, low_s, weight_blocks(place_ref, weights, far_ref))
    for pair in range(2):
        at = pl.multiple_of(((place_ref[0] & 1) ^ pair) * width, width)
        out_ref[:, pl.ds(at, width)] = value[:, pair * width : (pair + 1) * width]
    for half in range(2):

        @pl.when(step == half)
        def _():
            first = 2 * half * width
            for (_, column), up in zip(spots, ups):
                low = max(column, first)
                high = min(column + up.shape[1], first + 2 * width)
                if low < high:
                    out_ref[:, low - first : high - first] += up[:, low - column : high - column]


def own_terms(columns, place, grad, ups, weights, layer):
    frames, features = grad.shape
    width = features // 4
    whole = lambda array: pl.BlockSpec(array.shape, lambda s, cols, place: (0,) * array.ndim)
    step_block = pl.BlockSpec((frames, 2 * width), lambda s, cols, place: (0, s))
    return call(
        partial(own_terms_body, len(ups), spots_of_sum(ups, width)),
        grid_spec=pltpu.PrefetchScalarGridSpec(
            num_scalar_prefetch=2,
            grid=(2,),
            in_specs=[whole(grad)]
            + [part_spec(up, frames) for up in ups]
            + weight_specs(weights, layer),
            out_specs=step_block,
            scratch_shapes=[pltpu.VMEM((4, frames, width), BF16)] * 2 + [far_scratch(width)],
        ),
        out_shape=jax.ShapeDtypeStruct((frames, features), F32),
        cost_estimate=cost(6 * frames * features * features, 4 * features * features),
        name="own_terms",
    )(columns, place, in_hbm(grad), *arrays_of(ups), *[in_hbm(w) for w in weights])


def prepare_body(lists_ref, place_ref, own_ref, near_ref, high_ref, low_ref):
    del lists_ref
    padded = high_ref.shape[0] // 2
    width = high_ref.shape[1] // 2
    for clip, part in enumerate((own_ref, near_ref)):
        rows = part.shape[0]
        for dc in range(2):
            at = pl.multiple_of((place_ref[6] ^ clip ^ dc) * width, width)
            high, low = split(part[:, dc * width : (dc + 1) * width])
            high_ref[clip * padded : clip * padded + rows, pl.ds(at, width)] = high
            low_ref[clip * padded : clip * padded + rows, pl.ds(at, width)] = low
        zeros = jnp.zeros((padded - rows, 2 * width), BF16)
        high_ref[clip * padded + rows : (clip + 1) * padded, :] = zeros
        low_ref[clip * padded + rows : (clip + 1) * padded, :] = zeros


def prepare(place, own, near):
    frames, features = own.shape
    width = features // 4
    padded = -(-frames // LANES) * LANES
    in_spec = pl.BlockSpec((frames, 2 * width), lambda s, *_: (0, s))
    out = jax.ShapeDtypeStruct((2 * padded, features), BF16)
    out_spec = pl.BlockSpec((2 * padded, 2 * width), lambda s, order, place: (0, order[s]))
    order = jnp.stack([place[0] >> 1, 1 - (place[0] >> 1)])
    return call(
        prepare_body,
        grid_spec=pltpu.PrefetchScalarGridSpec(
            num_scalar_prefetch=2,
            grid=(2,),
            in_specs=[in_spec, in_spec],
            out_specs=[out_spec, out_spec],
        ),
        out_shape=[out, out],
        hbm_outs=(0, 1),
        cost_estimate=cost(0, 16 * frames * features),
        name="prepare",
    )(order, place, in_hbm(own), in_hbm(near))


def product(g_high, g_low, x_high, x_low):
    return dot(g_high, x_high, NN) + (dot(g_high, x_low, NN) + dot(g_low, x_high, NN))


def weight_body(turn, place_ref, *refs):
    if turn:
        grad_ref, near_ref, x_high, x_low, kept, sent, g_high, g_low, t_high, t_low = refs

        @pl.when(pl.program_id(0) == 0)
        def _():
            frames, features = grad_ref.shape
            width = features // 4
            rows = width // 4
            padded = t_high.shape[1] // 2
            t_high[...] = jnp.zeros_like(t_high)
            t_low[...] = jnp.zeros_like(t_low)
            for clip in range(2):
                for dh in range(2):
                    if clip == 0:
                        part = grad_ref[:, 2 * dh * width : (2 * dh + 1) * width]
                    else:
                        part = near_ref[:, dh * width : (dh + 1) * width]
                    high, low = split(part.T)
                    at = (
                        slice(dh * width, (dh + 1) * width),
                        slice(clip * padded, clip * padded + frames),
                    )
                    t_high[at] = high
                    t_low[at] = low
            for group in range(8):
                first, second, dh = group // 4, group // 2 % 2, group % 2
                core = place_ref[6]
                y = place_ref[4] ^ (first * core + second * (1 - core))
                x = place_ref[5] ^ (first * (1 - core) + second * core)
                at = pl.multiple_of(dh * width + (2 * y + x) * rows, rows)
                g_high[group * rows : (group + 1) * rows, :] = t_high[pl.ds(at, rows), :]
                g_low[group * rows : (group + 1) * rows, :] = t_low[pl.ds(at, rows), :]

    else:
        g_high, g_low, x_high, x_low, kept, sent = refs
    half = g_high.shape[0] // 2
    value = product(g_high[...], g_low[...], x_high[...], x_low[...])
    kept[...] = value[:half].reshape(kept.shape)
    sent[...] = value[half:].reshape(sent.shape)


def weight_rows(side, place, grads, x_split, width):
    turn = side == 0
    whole = lambda array: pl.BlockSpec(array.shape, lambda s, place: (0,) * array.ndim)
    x_spec = pl.BlockSpec((x_split[0].shape[0], width), lambda s, place: (0, s))
    shape = (2, 2, width // 4, 4 * width)
    out_shape = [jax.ShapeDtypeStruct(shape, F32)] * 2
    out_specs = [pl.BlockSpec(shape[:3] + (width,), lambda s, place: (0, 0, 0, s))] * 2
    scratch = []
    if turn:
        turned = (2 * width, x_split[0].shape[0])
        out_shape += [jax.ShapeDtypeStruct(turned, BF16)] * 2
        out_specs += [whole(out_shape[-1])] * 2
        scratch = [pltpu.VMEM(turned, BF16)] * 2
    return call(
        partial(weight_body, turn),
        grid_spec=pltpu.PrefetchScalarGridSpec(
            num_scalar_prefetch=1,
            grid=(4,),
            in_specs=[whole(a) for a in grads] + [x_spec] * 2,
            out_specs=out_specs,
            scratch_shapes=scratch,
        ),
        out_shape=out_shape,
        hbm_outs=(0,),
        cost_estimate=cost(12 * x_split[0].shape[0] * width * 4 * width, 4 * 8 * width * width),
        name="weight_rows",
    )(place, *([in_hbm(grads[0]), grads[1]] if turn else grads), *[in_hbm(x) for x in x_split])


def step_body(n, widths, cut, *refs):
    ins, outs = refs[: 2 * n], refs[2 * n :]
    starts = [sum(widths[:i]) for i in range(len(widths))]
    column = 0
    for i in range(n):
        total = ins[2 * i][...] + ins[2 * i + 1][...]
        end = column + total.shape[-1]
        for j, (start, columns) in enumerate(zip(starts, widths)):
            low, high = max(start, column), min(start + columns, end)
            if low < high:
                to = (Ellipsis, slice(low - start, high - start))
                piece = total[..., low - column : high - column]
                pieces = [piece]
                for _ in range(cut):
                    pieces = [half[k] for half in pieces for k in range(2)]
                for k, some in enumerate(pieces):
                    outs[len(pieces) * j + k][to] = some
        column = end


def step_of(*pairs, cut=1, widths=None, hbm_outs=()):
    shape = list(pairs[0][0].shape)
    widths = widths or [sum(pair[0].shape[-1] for pair in pairs)]
    outs = []
    for columns in widths:
        shape[-1] = columns
        outs += [jax.ShapeDtypeStruct(tuple(shape[cut:]), F32)] * 2**cut
    whole = lambda array: pl.BlockSpec(array.shape, lambda i: (0,) * array.ndim)
    operands = [array for pair in pairs for array in pair]
    return call(
        partial(step_body, len(pairs), widths, cut),
        grid=(1,),
        in_specs=[whole(a) for a in operands],
        out_specs=[whole(a) for a in outs],
        out_shape=outs,
        hbm_outs=hbm_outs,
        cost_estimate=cost(0, 4 * sum(a.size for a in operands)),
        name="reduction_step",
    )(*operands)


def plane_swap(array, step):
    pairs = []
    for i in range(8):
        over_x = (i % 2 == 0) == (step == 0)
        pairs.append((i, i ^ 2 if over_x else i ^ 4))
    return lax.ppermute(array, ("y", "x", "c"), pairs)


def plane_gather(share, *before):
    first = plane_swap(share, 0)
    second = plane_swap(share, 1)
    return [share, second, first, plane_swap(after(first, second, *before), 1)]


def assemble_body(place_ref, *refs):
    out_ref = refs[-1]
    core = place_ref[6]
    rows, columns = refs[0].shape
    quarter = columns // 4
    for i in range(4):
        first, second = i // 2, i % 2
        y = place_ref[4] ^ (first * core + second * (1 - core))
        x = place_ref[5] ^ (first * (1 - core) + second * core)
        at = pl.multiple_of((2 * y + x) * rows, rows)
        for side in range(2):
            for h in range(2):
                to = pl.multiple_of((2 * h + (place_ref[7] ^ side)) * quarter, quarter)
                some = slice((2 * side + h) * quarter, (2 * side + h + 1) * quarter)
                out_ref[0, pl.ds(at, rows), pl.ds(to, quarter)] = refs[i][:, some]


def assemble(place, pieces, layer, onto=None):
    rows, columns = 4 * pieces[0].shape[0], pieces[0].shape[1]
    aliases, extra, extra_specs = {}, [], []
    if onto is not None:
        aliases, extra = {1 + len(pieces): 0}, [onto]
        extra_specs = [pl.BlockSpec(memory_space=pl.ANY)]
    (out,) = call(
        assemble_body,
        grid=(1,),
        out_shape=[jax.ShapeDtypeStruct((LAYERS, rows, columns), F32)],
        hbm_outs=(0,),
        in_specs=[SMEM_SPEC]
        + [pl.BlockSpec(p.shape, lambda i: (0, 0)) for p in pieces]
        + extra_specs,
        out_specs=[pl.BlockSpec((1, rows, columns), lambda i: (layer, 0, 0))],
        input_output_aliases=aliases,
        cost_estimate=cost(0, 8 * rows * columns),
        name="assemble",
    )(place, *[p if extra else in_hbm(p) for p in pieces], *extra)
    return out


def half_features(inputs, weights, gains, shifts, decays, biases, lengths, frame_mask, grad_out):
    width, slots = inputs.shape
    clips, frames = frame_mask.shape
    depth = weights.shape[2]
    blocks = 4 * width // LANES
    y, x, h, l, c = (lax.axis_index(name) for name in ("y", "x", "h", "l", "c"))
    b = 2 * y + x
    numbers = [2 * (h ^ (rel // 2)) + (c ^ (rel % 2)) for rel in range(4)] + [y, x, c, l]
    place = jnp.stack(numbers).astype(jnp.int32)
    own_blocks, other_blocks = (
        jnp.stack(
            [2 * (2 * (h ^ (rel // 2)) + half) + (c ^ (rel % 2)) for rel in range(4)]
        ).astype(jnp.int32)
        for half in (l, 1 - l)
    )
    own_columns = jnp.stack([2 * h + l, 2 * (1 - h) + l]).astype(jnp.int32)
    other_columns = jnp.stack([2 * (1 - h) + 1 - l, 2 * h + 1 - l]).astype(jnp.int32)
    rows = width // 4

    clip = 2 * h + c
    seen = lax.dynamic_index_in_dim(frame_mask, clip, 0, keepdims=False)
    length = lax.dynamic_index_in_dim(lengths, clip, 0, keepdims=False)
    moments = jnp.arange(frames, dtype=jnp.int32)
    gate = ((moments < length) & ((seen == 1) | (moments == 0))).astype(F32)
    valid = jnp.broadcast_to(gate[:, None], (frames, LANES))

    def far_share(layer):
        return lax.dynamic_slice(weights, (layer, b * rows, 0), (1, rows, depth))[0]

    def over_h(array):
        return lax.ppermute(array, "h", FLIP2)

    def over_c(array):
        return lax.ppermute(array, "c", FLIP2)

    def over_second(array):
        return plane_swap(array, 1)

    def four_of(near_rows, far_rows):
        return [
            (near_rows, 0),
            (over_c(near_rows), 1),
            (far_rows, 0),
            (over_c(far_rows), 1),
        ]

    def four_of_plane(share):
        both = lax.ppermute(share, ("y", "x"), DIAGONAL)
        return [share, lax.ppermute(share, "x", FLIP2), lax.ppermute(share, "y", FLIP2), both]

    near = over_c(weights)
    share = far_share(0)
    close, away = pack(place, after(inputs, share), frames)
    share = over_h(share)
    away = over_h(away)
    other_close = swap_half(close)
    up_close, up_away = pack(place, after(grad_out, close), frames, waits=True)
    share = after(share, up_close, valid, near, other_close)
    pieces = four_of_plane(share)
    away = after(away, pieces[1:])
    half_weights = [[weights, near, *pieces, *map(over_c, after(pieces, away))]]
    own = four_of(after(close, away), away)
    other_away = swap_half(away)
    others = [(other_close, 0), (over_c(other_close), 1)]
    params = jnp.stack([gains, shifts + biases, decays], axis=1)
    own_params = params.reshape(LAYERS * 3 * width // LANES, LANES)
    params = None

    def gather(array, axes):
        return lax.all_gather(array, axes, tiled=True)

    weight = half_weights[0]
    early = jnp.concatenate([own_blocks, other_blocks[:2]])
    z, own_flat = project(place, frames, own + others, early, weight, 0, flat=own)
    others += [(other_away, 0), (over_c(after(other_away, z)), 1)]
    z, stats, other_flat = project(
        place,
        frames,
        others[2:],
        other_blocks[2:],
        weight,
        0,
        z,
        valid,
        params=own_params,
        flat=others,
    )
    z = [z]
    stats = gather(stats, ("h", "c"))
    share = over_c(lax.ppermute(after(far_share(1), stats), ("h", "c"), DIAGONAL))
    stats = gather(stats, ("y", "x"))
    x, states, slopes, params = recur(0, place, gate, z, stats, None, valid, own_flat, False)
    own_near, other_near = over_c(after(own_flat, z[0])), over_c(after(other_flat, z[0]))
    x_near = over_c(x)
    own_split = prepare(place, after(own_flat, x_near), own_near)
    other_split = prepare(place, after(other_flat, x_near), other_near)
    saved = [(own_split, other_split, z, stats, states, slopes)]

    pieces = four_of_plane(after(share, slopes, own_near, other_near))
    near = [weights, near]
    other = swap_half(x)
    x_own = after(x, own_split[0], other_split[0])
    z, *_ = project(place, frames, [(x_own, None)], own_blocks, near, 1)
    own_split = prepare(place, after(x, z), x_near)
    far = [*pieces, *map(over_c, after(pieces, own_split[0]))]
    up_away = over_h(after(up_away, other, own_split[0]))
    half_weights.append(near + far)
    z, stats = project(place, frames, [(other, None)], other_blocks, near, 1, z, valid)
    both = jnp.concatenate([own_blocks, other_blocks])
    z_far, stats = project(
        place,
        frames,
        [(x, None), (other, None)],
        both,
        far,
        1,
        None,
        valid,
        stats,
    )
    z = [z, z_far]
    stats = gather(gather(stats, ("y", "x")), ("h", "c"))
    upstream = four_of(up_close, after(up_away, stats))
    *output, states, slopes = recur(1, place, gate, z, stats, params, valid, x, True)
    other_near = over_c(after(other, slopes))
    saved.append((own_split, (other, other_near), z, stats, states, slopes))
    diagonal = over_c(over_h(output[3]))

    ups = upstream
    results = [None] * LAYERS
    for layer in range(LAYERS - 1, -1, -1):
        own_split, other_split, z, stats, states, slopes = saved[layer]
        weight = half_weights[layer]
        grad_pre, sums = back(layer, place, gate, z, stats, params, ups, states, slopes)
        sums = gather(sums, ("y", "x"))
        if layer == 0:
            come[0] = after(come[0], sums, away, output[1][0])
            later, go = step_of((in_hbm(stay[0]), come[0]), (in_hbm(stay[1]), come[1]))
            sums = after(sums, later)
            go = over_second(go)
        sums = gather(sums, ("h", "c"))
        grad_z, leaving, *terms, sums = norm_back(
            other_columns, place, grad_pre, z, params, valid, stats, sums, weight, layer,
            layer == 0,
        )
        leaving = over_c(leaving)
        if layer > 0:
            received = [swap_half(terms[0])]
            other_split = prepare(place, *after(other_split, grad_z))
            leaving = after(leaving, diagonal, other_split[0])
        else:
            received = [None, swap_half(terms[1])]
            later, go = step_of((later, after(go, grad_z)), hbm_outs=(0,))
            leaving = after(leaving, later)
            go = lax.ppermute(go, ("h", "c"), DIAGONAL)
            later = (later, go)
        *first, g_high, g_low = weight_rows(0, place, (grad_z, leaving), own_split, width)
        turned = (g_high, g_low)
        come = [plane_swap(first[1], 0)]
        if layer == 0:
            received[0] = swap_half(after(terms[0], received[1]))
        second = weight_rows(1, place, turned, other_split, width)
        come.append(plane_swap(second[1], 0))
        stay = (first[0], second[0])
        kept = own_terms(own_columns, place, after(grad_z, second[0]), ups, weight, layer)
        if layer > 0:
            away = over_h(after(output[2], kept))
            output = [(a, 0) for a in (output[0], over_c(output[1]), away, diagonal)]
        ups = [(kept, None)] + [(r, None) for r in received]
        results[layer] = lax.dynamic_index_in_dim(
            sums.reshape(3, 4, width), clip, axis=1, keepdims=False
        )

    sums = jnp.stack(results)
    sums = [sums[:, 0], sums[:, 1], sums[:, 2]]
    aways = merge(kept, 1, received[1], apart=True)
    later = (in_hbm(later[0]), over_c(after(later[1], aways[0])))
    come[0] = after(come[0], sums, later[1])
    far_near = over_c(lax.ppermute(aways[0], ("h", "c"), DIAGONAL))
    near_sum, far_sum, near_go, far_go = step_of(
        (in_hbm(stay[0]), come[0]), (in_hbm(stay[1]), come[1]), cut=2
    )
    near_go, far_go = over_second(near_go), over_second(far_go)
    (go,) = step_of((far_sum, after(far_go, far_near)), cut=0)
    (later,) = step_of(later, cut=0)
    later = after(later, go)
    go = over_h(go)
    later = plane_gather(later)
    (total,) = step_of((near_sum, near_go), cut=0)
    output = unpack(place, [(after(array, total), i) for array, i in output], frames, waited=True)
    close = merge(kept, 0, after(received[0], output))
    far = over_c(over_h(after(aways[1], go)))
    (share,) = step_of((total, after(go, close, *later[1:])), cut=0)
    grad_weights = assemble(place, after(later, share), 1)
    gathered = plane_gather(share, grad_weights)
    grad_in = [(close, 0), (over_c(close[frames:]), 0), (far_near, 0), (far, 0)]
    grad_in = unpack(place, grad_in, frames)
    grad_weights = assemble(place, after(gathered, grad_in), 0, grad_weights)
    return (output, grad_in, grad_weights, *sums, sums[1])


def gelu_slope(value):
    return (
        0.5 * (1.0 + jax.scipy.special.erf(value / ROOT_TWO))
        + value * jnp.exp(-0.5 * value * value) / ROOT_TWO_PI
    )


def recur_step(decay, state, inputs):
    drive_t, valid_t = inputs
    pre = drive_t + decay * state
    state = state + valid_t * (jax.nn.gelu(pre, approximate=False) - state)
    return (state, state)


def back_step(decay, carry, inputs):
    upstream_t, valid_t, pre_t = inputs
    total = upstream_t + carry
    grad_pre = total * valid_t * gelu_slope(pre_t)
    carry = total * (1.0 - valid_t) + grad_pre * decay
    return (carry, grad_pre)


def add_piece(weight, piece):
    return jnp.dot(weight, piece, precision=HIGH, preferred_element_type=jnp.float32)


def weight_columns(grad_pre_norm, piece):
    return jnp.einsum("jf,kf->jk", grad_pre_norm, piece, precision=HIGH)


def split_features(inputs, weights, gains, shifts, decays, biases, lengths, frame_mask, grad_out):
    width, slots = inputs.shape
    clips, frames_len = frame_mask.shape
    frames = jnp.arange(frames_len, dtype=jnp.int32)
    valid_grid = (
        (frames[None, :] < lengths[:, None]) & ((frame_mask == 1) | (frames[None, :] == 0))
    ).astype(jnp.float32)
    valid = valid_grid.reshape(-1)
    valid_row = valid[None, :]
    valid_time = jnp.broadcast_to(valid_grid.T[:, :, None], (frames_len, clips, width)).reshape(
        frames_len, clips * width
    )
    count_local = jnp.sum(valid)

    def to_time(array):
        return jnp.transpose(array.reshape(width, clips, frames_len), (2, 1, 0)).reshape(
            frames_len, clips * width
        )

    def from_time(array):
        return jnp.transpose(array.reshape(frames_len, clips, width), (2, 1, 0)).reshape(
            width, slots
        )

    layer_in = inputs
    saved = []
    for layer_no in range(LAYERS):
        weight = weights[layer_no]
        gathered = lax.all_gather(layer_in, "neuron", axis=0, tiled=True)
        pre_norm = add_piece(weight, gathered)
        first_sum, count = lax.psum((jnp.sum(valid_row * pre_norm, axis=1), count_local), "batch")
        mean = first_sum / count
        centered = pre_norm - mean[:, None]
        var = lax.psum(jnp.sum(valid_row * centered * centered, axis=1), "batch") / count
        inv_std = lax.rsqrt(var + EPS)
        zhat = (pre_norm - mean[:, None]) * inv_std[:, None]
        drive = gains[layer_no][:, None] * zhat + (shifts[layer_no] + biases[layer_no])[:, None]
        drive_time = to_time(drive)
        decay_wide = jnp.tile(decays[layer_no], clips)
        start_state = jnp.zeros((clips * width,), jnp.float32)
        _, states = lax.scan(
            partial(recur_step, decay_wide), start_state, (drive_time, valid_time), unroll=8
        )
        saved.append((gathered, zhat, inv_std, drive_time, states, count))
        layer_in = layer_in + valid_row * from_time(states)
    upstream = grad_out
    grad_parts = [None] * LAYERS
    for layer_no in range(LAYERS - 1, -1, -1):
        gathered, zhat, inv_std, drive_time, states, count = saved[layer_no]
        decay_wide = jnp.tile(decays[layer_no], clips)
        gain = gains[layer_no]
        previous = jnp.concatenate([jnp.zeros_like(states[:1]), states[:-1]], axis=0)
        pre_time = drive_time + decay_wide[None, :] * previous
        grad_state = to_time(valid_row * upstream)
        start_carry = jnp.zeros((clips * width,), jnp.float32)
        _, grad_pre_time = lax.scan(
            partial(back_step, decay_wide),
            start_carry,
            (grad_state, valid_time, pre_time),
            reverse=True,
            unroll=8,
        )
        decay_local = jnp.sum(
            jnp.sum(grad_pre_time * previous, axis=0).reshape(clips, width), axis=0
        )
        grad_pre = from_time(grad_pre_time)
        gain_local = jnp.sum(grad_pre * zhat, axis=1)
        shift_local = jnp.sum(grad_pre, axis=1)
        grad_gain, grad_shift, grad_decay = lax.psum(
            (gain_local, shift_local, decay_local), "batch"
        )
        grad_pre_norm = (gain * inv_std)[:, None] * (
            grad_pre - valid_row * (grad_shift[:, None] + zhat * grad_gain[:, None]) / count
        )
        weight_local = weight_columns(grad_pre_norm, gathered)
        input_terms = jnp.einsum("jk,jf->kf", weights[layer_no], grad_pre_norm, precision=HIGH)
        input_grad = lax.psum_scatter(input_terms, "neuron", scatter_dimension=0, tiled=True)
        grad_weight = lax.psum(weight_local, "batch")
        upstream = upstream + input_grad
        grad_parts[layer_no] = (grad_weight, grad_gain, grad_shift, grad_decay)
    grad_weights = jnp.stack([grad_parts[layer_no][0] for layer_no in range(LAYERS)])
    grad_gains = jnp.stack([grad_parts[layer_no][1] for layer_no in range(LAYERS)])
    grad_shifts = jnp.stack([grad_parts[layer_no][2] for layer_no in range(LAYERS)])
    grad_decays = jnp.stack([grad_parts[layer_no][3] for layer_no in range(LAYERS)])
    return (layer_in, upstream, grad_weights, grad_gains, grad_shifts, grad_decays, grad_shifts)


def solution(mesh):
    if (mesh.shape["batch"], mesh.shape["neuron"]) == (4, 8):
        cut = Mesh(mesh.devices.reshape(2, 2, 2, 2, 2), ("y", "x", "h", "l", "c"))
        batch, neuron, body = ("y", "x"), ("h", "l", "c"), half_features
    else:
        cut, batch, neuron, body = mesh, "batch", "neuron", split_features
    in_specs = (
        P(neuron, batch),
        P(None, neuron, None),
        P(None, neuron),
        P(None, neuron),
        P(None, neuron),
        P(None, neuron),
        P(batch),
        P(batch, None),
        P(neuron, batch),
    )
    out_specs = (
        P(neuron, batch),
        P(neuron, batch),
        P(None, neuron, None),
        P(None, neuron),
        P(None, neuron),
        P(None, neuron),
        P(None, neuron),
    )
    return jax.shard_map(
        body, mesh=cut, in_specs=in_specs, out_specs=out_specs, check_vma=False
    )
```

```python
from functools import partial
import math

import jax
import jax.numpy as jnp
from jax import lax
from jax.experimental import pallas as pl
from jax.experimental.pallas import tpu as pltpu
from jax.sharding import Mesh, PartitionSpec as P

LAYERS = 2
EPS = 1e-05
HIGH = lax.Precision.HIGHEST
ROOT_TWO = math.sqrt(2.0)
ROOT_TWO_PI = math.sqrt(2.0 * math.pi)
F32 = jnp.float32
BF16 = jnp.bfloat16
LANES = 128
VMEM_LIMIT = 24 * 1024 * 1024
SMEM_SPEC = pl.BlockSpec(memory_space=pltpu.SMEM)
VMEM_SPEC = pl.BlockSpec(memory_space=pltpu.VMEM)


FLIP2 = [(0, 1), (1, 0)]
DIAGONAL = [(0, 3), (1, 2), (2, 1), (3, 0)]


def swap_half(array):
    return lax.ppermute(array, "l", FLIP2)


def after(value, *others):
    return lax.optimization_barrier((value, others))[0]


def split(value):
    high = value.astype(BF16)
    return high, (value - high.astype(F32)).astype(BF16)


def dot(a, b, dims):
    return lax.dot_general(a, b, (dims, ((), ())), preferred_element_type=F32)


NT = ((1,), (1,))
NN = ((1,), (0,))


def in_hbm(array):
    return pltpu.with_memory_space_constraint(array, pltpu.HBM)


def call(body, out_shape, hbm_outs=(), **kwargs):
    if hbm_outs:
        out_shape = [
            pltpu.HBM(a.shape, a.dtype) if i in hbm_outs else a for i, a in enumerate(out_shape)
        ]
    return pl.pallas_call(
        body,
        out_shape=out_shape,
        compiler_params=pltpu.CompilerParams(vmem_limit_bytes=VMEM_LIMIT),
        **kwargs,
    )


def cost(flops, byte_count):
    return pl.CostEstimate(flops=int(flops) // 64, bytes_accessed=int(byte_count) // 64, transcendentals=0)


def pack_body(frames, place_ref, in_ref, near_ref, far_ref, turned):
    slots = in_ref.shape[1]
    for start in range(0, slots, LANES):
        turned[start : start + LANES, :] = in_ref[:, start : start + LANES].T
    for rel in range(4):
        first = pl.multiple_of(place_ref[rel] * frames, 8)
        out = (near_ref, far_ref)[rel // 2]
        out[(rel % 2) * frames : (rel % 2 + 1) * frames, :] = turned[pl.ds(first, frames), :]


def pack(place, array, frames, waits=False):
    width, slots = array.shape
    out = jax.ShapeDtypeStruct((2 * frames, width), F32)
    return call(
        partial(pack_body, frames),
        grid=(1,),
        out_shape=[out, out],
        in_specs=[SMEM_SPEC, pl.BlockSpec((width, slots), lambda i: (0, 0))],
        out_specs=[pl.BlockSpec(out.shape, lambda i: (0, 0))] * 2,
        scratch_shapes=[pltpu.VMEM((slots, width), F32)],
        hbm_outs=(0, 1) if waits else (),
        cost_estimate=cost(0, 8 * width * slots),
        name="pack",
    )(place, in_hbm(array))


def part_spec(part, frames):
    array, i = part
    if i is None:
        return pl.BlockSpec(array.shape, lambda *_: (0,) * array.ndim)
    return pl.BlockSpec((frames, array.shape[1]), lambda *_: (i, 0))


def arrays_of(parts):
    return [array for array, _ in parts]


def unpack_body(frames, place_ref, *refs):
    ins, out_ref, turned = refs[:4], refs[4], refs[5]
    slots = out_ref.shape[1]
    for rel in range(4):
        first = pl.multiple_of(place_ref[rel] * frames, 8)
        turned[pl.ds(first, frames), :] = ins[rel][...]
    for start in range(0, slots, LANES):
        out_ref[:, start : start + LANES] = turned[start : start + LANES, :].T


def unpack(place, parts, frames, waited=False):
    width = parts[0][0].shape[1]
    slots = 4 * frames
    return call(
        partial(unpack_body, frames),
        grid=(1,),
        out_shape=jax.ShapeDtypeStruct((width, slots), F32),
        in_specs=[SMEM_SPEC] + [part_spec(part, frames) for part in parts],
        out_specs=pl.BlockSpec((width, slots), lambda i: (0, 0)),
        scratch_shapes=[pltpu.VMEM((slots, width), F32)],
        cost_estimate=cost(0, 8 * width * slots),
        name="unpack",
    )(place, *[in_hbm(a) if waited else a for a in arrays_of(parts)])


def merge_body(kept_ref, come_ref, *outs):
    frames, columns = kept_ref.shape
    width = columns // 2
    for i in range(2):
        some = slice(i * width, (i + 1) * width)
        if len(outs) > 1:
            outs[i][...] = kept_ref[:, some] + come_ref[:, some]
            continue
        (out_ref,) = outs
        out_ref[i * frames : (i + 1) * frames, :] = kept_ref[:, some] + come_ref[:, some]


def merge(kept, half, come, apart=False):
    frames, columns = come.shape
    rows, n = (frames, 2) if apart else (2 * frames, 1)
    outs = call(
        merge_body,
        hbm_outs=(0, 1) if apart else (),
        grid=(1,),
        out_shape=[jax.ShapeDtypeStruct((rows, columns // 2), F32)] * n,
        in_specs=[
            pl.BlockSpec((frames, columns), lambda i: (0, half)),
            pl.BlockSpec((frames, columns), lambda i: (0, 0)),
        ],
        out_specs=[pl.BlockSpec((rows, columns // 2), lambda i: (0, 0))] * n,
        cost_estimate=cost(0, 12 * frames * columns),
        name="merge",
    )(kept, come)
    return outs if apart else outs[0]


def project_body(n_parts, n_flat, spots, n_weights, first, with_acc, with_stats, with_params, cols_ref, place_ref, *refs):
    del cols_ref

    def take(n):
        nonlocal refs
        some, refs = refs[:n], refs[n:]
        return some

    parts, flat_parts, weights = take(n_parts), take(n_flat), take(n_weights)
    acc, valid, stats_in, params = take(with_acc), take(with_stats > 0), take(with_stats > 1), take(with_params)
    (out_ref,) = take(1)
    stats, flat = take(with_stats > 0), take(n_flat > 0)
    x_high, x_low, far_ref = refs
    step = pl.program_id(0)
    width = x_high.shape[2]

    @pl.when(step == 0)
    def _():
        for block, part in zip(spots, parts):
            for start in range(0, part.shape[1], width):
                high, low = split(part[:, start : start + width])
                x_high[block + start // width] = high
                x_low[block + start // width] = low
        column = 0
        for part in flat_parts:
            flat[0][:, column : column + part.shape[1]] = part[...]
            column += part.shape[1]
        if with_acc:
            out_ref[...] = acc[0][...]
        else:
            out_ref[...] = jnp.zeros_like(out_ref)

    stacked = jnp.concatenate([x_high[step], x_low[step], x_high[step]], axis=1)
    for block, weight in enumerate(weight_blocks(place_ref, weights, far_ref)):
        w_high, w_low = split(weight)
        columns = slice(block * width, (block + 1) * width)
        out_ref[:, columns] += dot(stacked, jnp.concatenate([w_high, w_high, w_low], axis=1), NT)

    if with_stats:
        (stats_ref,) = stats

        @pl.when(step == pl.num_programs(0) - 1)
        def _():
            if stats_in:
                stats_ref[...] = stats_in[0][...]
            own = jnp.sum(valid[0][...], axis=0, keepdims=True)
            per = width // LANES
            for row in range(out_ref.shape[1] // LANES):
                z = out_ref[:, row * LANES : (row + 1) * LANES]
                total = jnp.sum(valid[0][...] * z, axis=0, keepdims=True)
                centred = valid[0][...] * (z - total / own)
                squares = jnp.sum(centred * centred, axis=0, keepdims=True)
                at = place_ref[first + row // per] * per + row % per
                stats_ref[0, pl.ds(at, 1), :] = total
                stats_ref[1, pl.ds(at, 1), :] = squares
                stats_ref[2, pl.ds(at, 1), :] = own
            if with_params:
                rest = params[0].shape[0] - 8
                stats_ref[3] = params[0][:8, :]
                stats_ref[4] = jnp.zeros_like(stats_ref[4])
                stats_ref[4, :rest, :] = params[0][8:, :]


def weight_specs(weights, layer, pairs=2):
    specs = []
    for weight in weights:
        if weight.ndim == 3:
            shape = (1, weight.shape[1], pairs * weight.shape[1])
            specs.append(pl.BlockSpec(shape, lambda s, cols, *_: (layer, 0, cols[s])))
        else:
            shape = (weight.shape[0], pairs * 4 * weight.shape[0])
            specs.append(pl.BlockSpec(shape, lambda s, cols, *_: (0, cols[s])))
    return specs


def far_scratch(width, pairs=2):
    return pltpu.VMEM((2, width, pairs * width), F32)


def weight_blocks(place_ref, refs, far_ref):
    near = [ref[0] for ref in refs if len(ref.shape) == 3]
    pieces = [ref for ref in refs if len(ref.shape) == 2]
    far = []
    for i in range(len(pieces) // 4):
        for rel, piece in enumerate(pieces[4 * i : 4 * i + 4]):
            rows = piece.shape[0]
            row = 2 * (place_ref[4] ^ (rel // 2)) + (place_ref[5] ^ (rel % 2))
            far_ref[i, pl.ds(pl.multiple_of(row * rows, rows), rows), :] = piece[...]
        far.append(far_ref[i])
    return near + far


def project(
    place, frames, parts, blocks, weights, layer, acc=None, valid=None, stats=None, params=None, flat=()
):
    near = weights[0].ndim == 3
    units = sum(1 if w.ndim == 3 else 0.25 for w in weights)
    width = weights[0].shape[1] if near else 4 * weights[0].shape[0]
    n = blocks.shape[0]
    spots, block = [], 0
    for array, _ in parts:
        spots.append(block)
        block += array.shape[1] // width
    full = pl.BlockSpec(memory_space=pltpu.VMEM)
    in_specs = [part_spec(part, frames) for part in (*parts, *flat)]
    in_specs += weight_specs(weights, layer, 1)
    operands = arrays_of(parts) + arrays_of(flat) + [in_hbm(w) for w in weights]
    array = jax.ShapeDtypeStruct((frames, int(units) * width), F32)
    array_spec = pl.BlockSpec(array.shape, lambda s, cols, place: (0, 0))
    out_shape, out_specs = [array], [array_spec]
    if acc is not None:
        in_specs.append(array_spec)
        operands.append(in_hbm(acc))
    if valid is not None:
        in_specs.append(full)
        operands.append(valid)
        shape = (3 if params is None else 5, 4 * width // LANES, LANES)
        out_shape.append(jax.ShapeDtypeStruct(shape, F32))
        out_specs.append(pl.BlockSpec(shape, lambda s, cols, place: (0, 0, 0)))
    for extra in (stats, params):
        if extra is not None:
            in_specs.append(full)
            operands.append(extra)
    if flat:
        out_shape.append(jax.ShapeDtypeStruct((frames, 4 * width), F32))
        out_specs.append(pl.BlockSpec((frames, 4 * width), lambda s, cols, place: (0, 0)))
    return call(
        partial(
            project_body,
            len(parts),
            len(flat),
            spots,
            len(weights),
            0 if near else 2,
            acc is not None,
            (valid is not None) + (stats is not None),
            params is not None,
        ),
        grid_spec=pltpu.PrefetchScalarGridSpec(
            num_scalar_prefetch=2,
            grid=(n,),
            in_specs=in_specs,
            out_specs=out_specs,
            scratch_shapes=[pltpu.VMEM((n, frames, width), BF16)] * 2 + [far_scratch(width, 1)],
        ),
        out_shape=out_shape,
        hbm_outs=(0, len(out_shape) - 1) if flat else (0,),
        cost_estimate=cost(6 * frames * n * width * units * width, 4 * n * width * units * width),
        name="project",
    )(blocks, place, *operands)


def to_relative(place_ref, spread, rows_ref, value, slot):
    per = value.shape[0] // 4
    spread[...] = value
    for rel in range(4):
        first = place_ref[rel] * per
        for row in range(per):
            rows_ref[slot, rel * per + row : rel * per + row + 1, :] = spread[
                pl.ds(first + row, 1), :
            ]


def tree(values):
    while len(values) > 1:
        values = [a + b for a, b in zip(values[::2], values[1::2])]
    return values[0]


def gathered(ref, slot):
    return [ref[i] for i in range(slot, ref.shape[0], ref.shape[0] // 16)]


def norm_terms(stats_ref):
    each = [gathered(stats_ref, slot) for slot in range(3)]
    totals, squares, owns = each
    count = tree(owns)
    mean = tree(totals) / count
    away = [total / own - mean for total, own in zip(totals, owns)]
    spread = tree([s + n * a * a for s, n, a in zip(squares, owns, away)])
    return count, mean, lax.rsqrt(spread / count + EPS)


CHUNKS = 4


def columns_of(refs, row):
    for ref in refs:
        if row * LANES < ref.shape[1]:
            return ref[:, row * LANES : (row + 1) * LANES]
        row -= ref.shape[1] // LANES


def recur_body(n_z, last, layer, spread_params, place_ref, gate_ref, *refs):
    z_refs, refs = refs[:n_z], refs[n_z:]
    (stats_ref, params_ref, valid_ref, x_ref), refs = refs[:4], refs[4:]
    outs, refs = refs[: 1 + 3 * last], refs[1 + 3 * last :]
    if spread_params:
        state_ref, slope_ref, params_out, rows, spread, held, drive_s, state_s, slope_s = refs
    else:
        state_ref, slope_ref, rows, spread, held, drive_s, state_s, slope_s = refs
    frames, features = x_ref.shape
    blocks = features // LANES
    per = blocks // 4
    chunk = pl.program_id(0)

    @pl.when(chunk == 0)
    def _():
        if spread_params:
            for rel in range(4):
                first = place_ref[rel] * (stats_ref.shape[0] // 16) + 3
                for row in range(LAYERS * 3 * per):
                    at = rel * per + row % per
                    params_out[row // per, at : at + 1, :] = stats_ref[
                        first + row // 8, row % 8 : row % 8 + 1, :
                    ]
            params = [params_out[3 * layer + i] for i in range(3)]
        else:
            params = [params_ref[3 * layer + i] for i in range(3)]
        _, mean, inv_std = norm_terms(stats_ref)
        to_relative(place_ref, spread, rows, mean, 0)
        to_relative(place_ref, spread, rows, inv_std, 1)
        rows[1] = rows[1] * params[0]
        rows[2] = params[1]
        rows[3] = params[2]
        held[...] = jnp.zeros_like(held)

    for row in range(blocks):
        drive_s[row * frames : (row + 1) * frames, :] = (
            columns_of(z_refs, row) - rows[0, row : row + 1, :]
        ) * rows[1, row : row + 1, :] + rows[2, row : row + 1, :]
    decay = rows[3]

    def step(t, state):
        at = pl.ds(t, blocks, stride=frames)
        pre = drive_s[at, :] + decay * state
        half = 0.5 + 0.5 * lax.erf(pre * (1.0 / ROOT_TWO))
        gate = gate_ref[chunk * frames + t] > 0.0
        slope = half + pre * jnp.exp(-0.5 * pre * pre) * (1.0 / ROOT_TWO_PI)
        state = jnp.where(gate, pre * half, state)
        state_s[at, :] = state
        slope_s[at, :] = jnp.where(gate, slope, 0.0)
        return state

    held[...] = lax.fori_loop(0, frames, step, held[...], unroll=8)
    valid = valid_ref[...]
    for row in range(blocks):
        lanes = slice(row * LANES, (row + 1) * LANES)
        state = state_s[row * frames : (row + 1) * frames, :]
        state_ref[:, lanes] = state
        slope_ref[:, lanes] = slope_s[row * frames : (row + 1) * frames, :]
        value = x_ref[:, lanes] + valid * state
        out, at = (outs[row // per], row % per) if last else (outs[0], row)
        out[:, at * LANES : (at + 1) * LANES] = value


def recur(layer, place, gate, z, stats, params, valid, x, last):
    frames, features = x.shape
    blocks = features // LANES
    some = frames // CHUNKS
    whole = lambda array: pl.BlockSpec(array.shape, lambda i: (0,) * array.ndim)
    by_chunk = lambda array: pl.BlockSpec((some, array.shape[1]), lambda i: (i, 0))
    full = jax.ShapeDtypeStruct((frames, features), F32)
    piece = jax.ShapeDtypeStruct((frames, features // 4), F32)
    out_shape = [piece] * 4 if last else [full]
    out_shape += [full, full]
    out_specs = [by_chunk(a) for a in out_shape]
    spread_params = params is None
    if spread_params:
        out_shape.append(jax.ShapeDtypeStruct((3 * LAYERS, blocks, LANES), F32))
        out_specs.append(whole(out_shape[-1]))
        params = valid
    return call(
        partial(recur_body, len(z), last, layer, spread_params),
        grid=(CHUNKS,),
        in_specs=[SMEM_SPEC, SMEM_SPEC]
        + [by_chunk(a) for a in z]
        + [whole(a) for a in (stats, params)]
        + [by_chunk(a) for a in (valid, x)],
        out_specs=out_specs,
        out_shape=out_shape,
        hbm_outs=tuple(range(len(out_shape) - spread_params)) if last else (1, 2),
        scratch_shapes=[
            pltpu.VMEM((4, blocks, LANES), F32),
            pltpu.VMEM((blocks, LANES), F32),
            pltpu.VMEM((blocks, LANES), F32),
        ]
        + [pltpu.VMEM((blocks * some, LANES), F32)] * 3,
        cost_estimate=cost(100 * frames * features, 20 * frames * features),
        name="recur",
    )(place, gate, *[in_hbm(a) for a in z], stats, params, valid, in_hbm(x))


def back_body(n_z, n_ups, spots, layer, place_ref, gate_ref, *refs):
    z_refs, refs = refs[:n_z], refs[n_z:]
    (stats_ref, params_ref), refs = refs[:2], refs[2:]
    ups, (state_ref, slope_ref), refs = refs[:n_ups], refs[n_ups : n_ups + 2], refs[n_ups + 2 :]
    grad_ref, sums_ref, rows, spread, held, up_s, state_s, slope_s = refs
    frames, features = state_ref.shape
    blocks = features // LANES
    per = blocks // 4
    tall = frames + 8
    step_no = pl.program_id(0)
    chunk = pl.num_programs(0) - 1 - step_no

    @pl.when(step_no == 0)
    def _():
        _, mean, inv_std = norm_terms(stats_ref)
        to_relative(place_ref, spread, rows, mean, 0)
        to_relative(place_ref, spread, rows, inv_std, 1)
        held[...] = jnp.zeros_like(held)

    for row in range(blocks):
        lanes = slice(row * LANES, (row + 1) * LANES)
        base = row * frames
        up = None
        for (_, column), part in zip(spots, ups):
            if column <= row * LANES < column + part.shape[1]:
                value = part[:, row * LANES - column : (row + 1) * LANES - column]
                up = value if up is None else up + value
        up_s[base : base + frames, :] = up
        state_s[row * tall : row * tall + 8, :] = jnp.zeros((8, LANES), F32)
        state_s[row * tall + 8 : (row + 1) * tall, :] = state_ref[:, lanes]
        slope_s[base : base + frames, :] = slope_ref[:, lanes]
    decay = params_ref[3 * layer + 2]

    def step(i, carry):
        t = frames - 1 - i
        at = pl.ds(t, blocks, stride=frames)
        slope = slope_s[at, :]
        gate = gate_ref[chunk * frames + t]
        total = gate * up_s[at, :] + carry
        up_s[at, :] = total * slope
        return total * (slope * decay + (1.0 - gate))

    held[0] = lax.fori_loop(0, frames, step, held[0], unroll=8)
    held[4] += held[1] * state_s[pl.ds(tall - 1, blocks, stride=tall), :]
    held[1] = up_s[pl.ds(0, blocks, stride=frames), :]
    for row in range(blocks):
        lanes = slice(row * LANES, (row + 1) * LANES)
        grad = up_s[row * frames : (row + 1) * frames, :]
        grad_ref[:, lanes] = grad
        zhat = (columns_of(z_refs, row) - rows[0, row : row + 1, :]) * rows[1, row : row + 1, :]
        before = state_s[row * tall + 7 : row * tall + 7 + frames, :]
        for slot, value in enumerate((grad * zhat, grad, grad * before)):
            held[2 + slot, row : row + 1, :] += jnp.sum(value, axis=0, keepdims=True)

    @pl.when(chunk == 0)
    def _():
        for row in range(blocks):
            at = place_ref[row // per] * per + row % per
            for slot in range(3):
                sums_ref[slot, pl.ds(at, 1), :] = held[2 + slot, row : row + 1, :]


def spots_of_sum(parts, width):
    spots, column = [], 0
    for array, _ in parts:
        spots.append((0, column % (4 * width)))
        column += array.shape[1]
    return spots


def back(layer, place, gate, z, stats, params, ups, states, slopes):
    frames, features = states.shape
    width = features // 4
    blocks = features // LANES
    some = frames // CHUNKS
    whole = lambda array: pl.BlockSpec(array.shape, lambda i: (0,) * array.ndim)

    def by_chunk(array, first=0):
        return pl.BlockSpec(
            (some, array.shape[1]), lambda i: ((first or 0) * CHUNKS + CHUNKS - 1 - i, 0)
        )

    out_shape = [
        jax.ShapeDtypeStruct((frames, features), F32),
        jax.ShapeDtypeStruct((3, blocks, LANES), F32),
    ]
    return call(
        partial(back_body, len(z), len(ups), spots_of_sum(ups, width), layer),
        grid=(CHUNKS,),
        in_specs=[SMEM_SPEC] * 2
        + [by_chunk(a) for a in z]
        + [whole(a) for a in (stats, params)]
        + [by_chunk(*up) for up in ups]
        + [by_chunk(a) for a in (states, slopes)],
        out_specs=[by_chunk(out_shape[0]), whole(out_shape[1])],
        out_shape=out_shape,
        scratch_shapes=[
            pltpu.VMEM((2, blocks, LANES), F32),
            pltpu.VMEM((blocks, LANES), F32),
            pltpu.VMEM((5, blocks, LANES), F32),
            pltpu.VMEM((blocks * some, LANES), F32),
            pltpu.VMEM((blocks * (some + 8), LANES), F32),
            pltpu.VMEM((blocks * some, LANES), F32),
        ],
        cost_estimate=cost(30 * frames * features, 20 * frames * features),
        name="back",
    )(
        place,
        gate,
        *[in_hbm(a) for a in z],
        stats,
        params,
        *arrays_of(ups),
        in_hbm(states),
        in_hbm(slopes),
    )


def input_terms(high_s, low_s, weights):
    left, right = [], []
    for block, weight in enumerate(weights):
        w_high, w_low = split(weight)
        left += [high_s[block], low_s[block], high_s[block]]
        right += [w_high, w_high, w_low]
    return dot(jnp.concatenate(left, axis=1), jnp.concatenate(right, axis=0), NN)


def norm_back_body(n_z, split_terms, layer, cols_ref, place_ref, grad_ref, *refs):
    del cols_ref
    z_refs, refs = refs[:n_z], refs[n_z:]
    params_ref, valid_ref, stats_ref, sums_ref, *refs = refs
    weights, refs = refs[:10], refs[10:]
    if split_terms:
        out_ref, leave_ref, near_term_ref, far_term_ref, sums_out_ref, *refs = refs
        term_refs, starts = (far_term_ref, near_term_ref), (0, 0)
    else:
        out_ref, leave_ref, term_ref, sums_out_ref, *refs = refs
        term_refs, starts = (term_ref, term_ref), (2 * grad_ref.shape[1] // 4, 0)
    rows, spread, high_s, low_s, far_ref = refs
    blocks = grad_ref.shape[1] // LANES
    width = high_s.shape[2]
    per = width // LANES

    @pl.when(pl.program_id(0) == 0)
    def _():
        count, mean, inv_std = norm_terms(stats_ref)
        to_relative(place_ref, spread, rows, mean, 0)
        to_relative(place_ref, spread, rows, inv_std, 1)
        rows[2] = rows[1] * params_ref[3 * layer]
        sums = [tree(gathered(sums_ref, slot)) for slot in range(3)]
        for slot in range(3):
            sums_out_ref[slot] = sums[slot]
        to_relative(place_ref, spread, rows, sums[0] / count, 3)
        to_relative(place_ref, spread, rows, sums[1] / count, 4)
        valid = valid_ref[...]
        for row in range(blocks):
            lanes = slice(row * LANES, (row + 1) * LANES)
            one = lambda slot: rows[slot, row : row + 1, :]
            zhat = (columns_of(z_refs, row) - one(0)) * one(1)
            value = one(2) * (grad_ref[:, lanes] - valid * (one(4) + zhat * one(3)))
            out_ref[:, lanes] = value
            if (row // per) % 2:
                at = (row // per // 2) * width + (row % per) * LANES
                leave_ref[:, at : at + LANES] = value
            high, low = split(value)
            inner = slice((row % per) * LANES, (row % per + 1) * LANES)
            high_s[row // per, :, inner] = high
            low_s[row // per, :, inner] = low

    value = input_terms(high_s, low_s, weight_blocks(place_ref, weights, far_ref))
    for step, (term_ref, first) in enumerate(zip(term_refs, starts)):

        @pl.when(pl.program_id(0) == step)
        def _():
            for pair in range(2):
                at = pl.multiple_of(((place_ref[0] & 1) ^ pair) * width, width)
                term_ref[:, pl.ds(first + at, width)] = value[
                    :, pair * width : (pair + 1) * width
                ]


def norm_back(columns, place, grad, z, params, valid, stats, sums, weights, layer, split_terms):
    frames, features = grad.shape
    width = features // 4
    blocks = features // LANES
    whole = lambda array: pl.BlockSpec(array.shape, lambda s, cols, place: (0,) * array.ndim)
    operands = [grad, *[in_hbm(a) for a in z], params, valid, stats, sums]
    full = jax.ShapeDtypeStruct((frames, features), F32)
    half = jax.ShapeDtypeStruct((frames, 2 * width), F32)
    terms = [half, half] if split_terms else [full]
    out_shape = [full, half, *terms, jax.ShapeDtypeStruct((3, blocks, LANES), F32)]
    return call(
        partial(norm_back_body, len(z), split_terms, layer),
        grid_spec=pltpu.PrefetchScalarGridSpec(
            num_scalar_prefetch=2,
            grid=(2,),
            in_specs=[whole(a) for a in operands] + weight_specs(weights, layer),
            out_specs=[whole(a) for a in out_shape],
            scratch_shapes=[
                pltpu.VMEM((5, blocks, LANES), F32),
                pltpu.VMEM((blocks, LANES), F32),
                pltpu.VMEM((4, frames, width), BF16),
                pltpu.VMEM((4, frames, width), BF16),
                far_scratch(width),
            ],
        ),
        out_shape=out_shape,
        hbm_outs=(0, 2) if split_terms else (0,),
        cost_estimate=cost(6 * frames * features * features, 4 * features * features),
        name="norm_back",
    )(columns, place, *operands, *[in_hbm(w) for w in weights])


def own_terms_body(n_ups, spots, cols_ref, place_ref, grad_ref, *refs):
    del cols_ref
    ups, refs = refs[:n_ups], refs[n_ups:]
    weights, refs = refs[:10], refs[10:]
    out_ref, high_s, low_s, far_ref = refs
    width = high_s.shape[2]
    step = pl.program_id(0)

    @pl.when(step == 0)
    def _():
        for block in range(4):
            high, low = split(grad_ref[:, block * width : (block + 1) * width])
            high_s[block] = high
            low_s[block] = low

    value = input_terms(high_s, low_s, weight_blocks(place_ref, weights, far_ref))
    for pair in range(2):
        at = pl.multiple_of(((place_ref[0] & 1) ^ pair) * width, width)
        out_ref[:, pl.ds(at, width)] = value[:, pair * width : (pair + 1) * width]
    for half in range(2):

        @pl.when(step == half)
        def _():
            first = 2 * half * width
            for (_, column), up in zip(spots, ups):
                low = max(column, first)
                high = min(column + up.shape[1], first + 2 * width)
                if low < high:
                    out_ref[:, low - first : high - first] += up[:, low - column : high - column]


def own_terms(columns, place, grad, ups, weights, layer):
    frames, features = grad.shape
    width = features // 4
    whole = lambda array: pl.BlockSpec(array.shape, lambda s, cols, place: (0,) * array.ndim)
    step_block = pl.BlockSpec((frames, 2 * width), lambda s, cols, place: (0, s))
    return call(
        partial(own_terms_body, len(ups), spots_of_sum(ups, width)),
        grid_spec=pltpu.PrefetchScalarGridSpec(
            num_scalar_prefetch=2,
            grid=(2,),
            in_specs=[whole(grad)]
            + [part_spec(up, frames) for up in ups]
            + weight_specs(weights, layer),
            out_specs=step_block,
            scratch_shapes=[pltpu.VMEM((4, frames, width), BF16)] * 2 + [far_scratch(width)],
        ),
        out_shape=jax.ShapeDtypeStruct((frames, features), F32),
        cost_estimate=cost(6 * frames * features * features, 4 * features * features),
        name="own_terms",
    )(columns, place, in_hbm(grad), *arrays_of(ups), *[in_hbm(w) for w in weights])


def prepare_body(lists_ref, place_ref, own_ref, near_ref, high_ref, low_ref):
    del lists_ref
    padded = high_ref.shape[0] // 2
    width = high_ref.shape[1] // 2
    for clip, part in enumerate((own_ref, near_ref)):
        rows = part.shape[0]
        for dc in range(2):
            at = pl.multiple_of((place_ref[6] ^ clip ^ dc) * width, width)
            high, low = split(part[:, dc * width : (dc + 1) * width])
            high_ref[clip * padded : clip * padded + rows, pl.ds(at, width)] = high
            low_ref[clip * padded : clip * padded + rows, pl.ds(at, width)] = low
        zeros = jnp.zeros((padded - rows, 2 * width), BF16)
        high_ref[clip * padded + rows : (clip + 1) * padded, :] = zeros
        low_ref[clip * padded + rows : (clip + 1) * padded, :] = zeros


def prepare(place, own, near):
    frames, features = own.shape
    width = features // 4
    padded = -(-frames // LANES) * LANES
    in_spec = pl.BlockSpec((frames, 2 * width), lambda s, *_: (0, s))
    out = jax.ShapeDtypeStruct((2 * padded, features), BF16)
    out_spec = pl.BlockSpec((2 * padded, 2 * width), lambda s, order, place: (0, order[s]))
    order = jnp.stack([place[0] >> 1, 1 - (place[0] >> 1)])
    return call(
        prepare_body,
        grid_spec=pltpu.PrefetchScalarGridSpec(
            num_scalar_prefetch=2,
            grid=(2,),
            in_specs=[in_spec, in_spec],
            out_specs=[out_spec, out_spec],
        ),
        out_shape=[out, out],
        hbm_outs=(0, 1),
        cost_estimate=cost(0, 16 * frames * features),
        name="prepare",
    )(order, place, in_hbm(own), in_hbm(near))


def product(g_high, g_low, x_high, x_low):
    return dot(g_high, x_high, NN) + (dot(g_high, x_low, NN) + dot(g_low, x_high, NN))


def weight_body(turn, place_ref, *refs):
    if turn:
        grad_ref, near_ref, x_high, x_low, kept, sent, g_high, g_low, t_high, t_low = refs

        @pl.when(pl.program_id(0) == 0)
        def _():
            frames, features = grad_ref.shape
            width = features // 4
            rows = width // 4
            padded = t_high.shape[1] // 2
            t_high[...] = jnp.zeros_like(t_high)
            t_low[...] = jnp.zeros_like(t_low)
            for clip in range(2):
                for dh in range(2):
                    if clip == 0:
                        part = grad_ref[:, 2 * dh * width : (2 * dh + 1) * width]
                    else:
                        part = near_ref[:, dh * width : (dh + 1) * width]
                    high, low = split(part.T)
                    at = (
                        slice(dh * width, (dh + 1) * width),
                        slice(clip * padded, clip * padded + frames),
                    )
                    t_high[at] = high
                    t_low[at] = low
            for group in range(8):
                first, second, dh = group // 4, group // 2 % 2, group % 2
                core = place_ref[6]
                y = place_ref[4] ^ (first * core + second * (1 - core))
                x = place_ref[5] ^ (first * (1 - core) + second * core)
                at = pl.multiple_of(dh * width + (2 * y + x) * rows, rows)
                g_high[group * rows : (group + 1) * rows, :] = t_high[pl.ds(at, rows), :]
                g_low[group * rows : (group + 1) * rows, :] = t_low[pl.ds(at, rows), :]

    else:
        g_high, g_low, x_high, x_low, kept, sent = refs
    half = g_high.shape[0] // 2
    value = product(g_high[...], g_low[...], x_high[...], x_low[...])
    kept[...] = value[:half].reshape(kept.shape)
    sent[...] = value[half:].reshape(sent.shape)


def weight_rows(side, place, grads, x_split, width):
    turn = side == 0
    whole = lambda array: pl.BlockSpec(array.shape, lambda s, place: (0,) * array.ndim)
    x_spec = pl.BlockSpec((x_split[0].shape[0], width), lambda s, place: (0, s))
    shape = (2, 2, width // 4, 4 * width)
    out_shape = [jax.ShapeDtypeStruct(shape, F32)] * 2
    out_specs = [pl.BlockSpec(shape[:3] + (width,), lambda s, place: (0, 0, 0, s))] * 2
    scratch = []
    if turn:
        turned = (2 * width, x_split[0].shape[0])
        out_shape += [jax.ShapeDtypeStruct(turned, BF16)] * 2
        out_specs += [whole(out_shape[-1])] * 2
        scratch = [pltpu.VMEM(turned, BF16)] * 2
    return call(
        partial(weight_body, turn),
        grid_spec=pltpu.PrefetchScalarGridSpec(
            num_scalar_prefetch=1,
            grid=(4,),
            in_specs=[whole(a) for a in grads] + [x_spec] * 2,
            out_specs=out_specs,
            scratch_shapes=scratch,
        ),
        out_shape=out_shape,
        hbm_outs=(0,),
        cost_estimate=cost(12 * x_split[0].shape[0] * width * 4 * width, 4 * 8 * width * width),
        name="weight_rows",
    )(place, *([in_hbm(grads[0]), grads[1]] if turn else grads), *[in_hbm(x) for x in x_split])


def step_body(n, widths, cut, *refs):
    ins, outs = refs[: 2 * n], refs[2 * n :]
    starts = [sum(widths[:i]) for i in range(len(widths))]
    column = 0
    for i in range(n):
        total = ins[2 * i][...] + ins[2 * i + 1][...]
        end = column + total.shape[-1]
        for j, (start, columns) in enumerate(zip(starts, widths)):
            low, high = max(start, column), min(start + columns, end)
            if low < high:
                to = (Ellipsis, slice(low - start, high - start))
                piece = total[..., low - column : high - column]
                pieces = [piece]
                for _ in range(cut):
                    pieces = [half[k] for half in pieces for k in range(2)]
                for k, some in enumerate(pieces):
                    outs[len(pieces) * j + k][to] = some
        column = end


def step_of(*pairs, cut=1, widths=None, hbm_outs=()):
    shape = list(pairs[0][0].shape)
    widths = widths or [sum(pair[0].shape[-1] for pair in pairs)]
    outs = []
    for columns in widths:
        shape[-1] = columns
        outs += [jax.ShapeDtypeStruct(tuple(shape[cut:]), F32)] * 2**cut
    whole = lambda array: pl.BlockSpec(array.shape, lambda i: (0,) * array.ndim)
    operands = [array for pair in pairs for array in pair]
    return call(
        partial(step_body, len(pairs), widths, cut),
        grid=(1,),
        in_specs=[whole(a) for a in operands],
        out_specs=[whole(a) for a in outs],
        out_shape=outs,
        hbm_outs=hbm_outs,
        cost_estimate=cost(0, 4 * sum(a.size for a in operands)),
        name="reduction_step",
    )(*operands)


def plane_swap(array, step):
    pairs = []
    for i in range(8):
        over_x = (i % 2 == 0) == (step == 0)
        pairs.append((i, i ^ 2 if over_x else i ^ 4))
    return lax.ppermute(array, ("y", "x", "c"), pairs)


def plane_gather(share, *before):
    first = plane_swap(share, 0)
    second = plane_swap(share, 1)
    return [share, second, first, plane_swap(after(first, second, *before), 1)]


def assemble_body(place_ref, *refs):
    out_ref = refs[-1]
    core = place_ref[6]
    rows, columns = refs[0].shape
    quarter = columns // 4
    for i in range(4):
        first, second = i // 2, i % 2
        y = place_ref[4] ^ (first * core + second * (1 - core))
        x = place_ref[5] ^ (first * (1 - core) + second * core)
        at = pl.multiple_of((2 * y + x) * rows, rows)
        for side in range(2):
            for h in range(2):
                to = pl.multiple_of((2 * h + (place_ref[7] ^ side)) * quarter, quarter)
                some = slice((2 * side + h) * quarter, (2 * side + h + 1) * quarter)
                out_ref[0, pl.ds(at, rows), pl.ds(to, quarter)] = refs[i][:, some]


def assemble(place, pieces, layer, onto=None):
    rows, columns = 4 * pieces[0].shape[0], pieces[0].shape[1]
    aliases, extra, extra_specs = {}, [], []
    if onto is not None:
        aliases, extra = {1 + len(pieces): 0}, [onto]
        extra_specs = [pl.BlockSpec(memory_space=pl.ANY)]
    (out,) = call(
        assemble_body,
        grid=(1,),
        out_shape=[jax.ShapeDtypeStruct((LAYERS, rows, columns), F32)],
        hbm_outs=(0,),
        in_specs=[SMEM_SPEC]
        + [pl.BlockSpec(p.shape, lambda i: (0, 0)) for p in pieces]
        + extra_specs,
        out_specs=[pl.BlockSpec((1, rows, columns), lambda i: (layer, 0, 0))],
        input_output_aliases=aliases,
        cost_estimate=cost(0, 8 * rows * columns),
        name="assemble",
    )(place, *[p if extra else in_hbm(p) for p in pieces], *extra)
    return out


def half_features(inputs, weights, gains, shifts, decays, biases, lengths, frame_mask, grad_out):
    width, slots = inputs.shape
    clips, frames = frame_mask.shape
    depth = weights.shape[2]
    blocks = 4 * width // LANES
    y, x, h, l, c = (lax.axis_index(name) for name in ("y", "x", "h", "l", "c"))
    b = 2 * y + x
    numbers = [2 * (h ^ (rel // 2)) + (c ^ (rel % 2)) for rel in range(4)] + [y, x, c, l]
    place = jnp.stack(numbers).astype(jnp.int32)
    own_blocks, other_blocks = (
        jnp.stack(
            [2 * (2 * (h ^ (rel // 2)) + half) + (c ^ (rel % 2)) for rel in range(4)]
        ).astype(jnp.int32)
        for half in (l, 1 - l)
    )
    own_columns = jnp.stack([2 * h + l, 2 * (1 - h) + l]).astype(jnp.int32)
    other_columns = jnp.stack([2 * (1 - h) + 1 - l, 2 * h + 1 - l]).astype(jnp.int32)
    rows = width // 4

    clip = 2 * h + c
    seen = lax.dynamic_index_in_dim(frame_mask, clip, 0, keepdims=False)
    length = lax.dynamic_index_in_dim(lengths, clip, 0, keepdims=False)
    moments = jnp.arange(frames, dtype=jnp.int32)
    gate = ((moments < length) & ((seen == 1) | (moments == 0))).astype(F32)
    valid = jnp.broadcast_to(gate[:, None], (frames, LANES))

    def far_share(layer):
        return lax.dynamic_slice(weights, (layer, b * rows, 0), (1, rows, depth))[0]

    def over_h(array):
        return lax.ppermute(array, "h", FLIP2)

    def over_c(array):
        return lax.ppermute(array, "c", FLIP2)

    def over_second(array):
        return plane_swap(array, 1)

    def four_of(near_rows, far_rows):
        return [
            (near_rows, 0),
            (over_c(near_rows), 1),
            (far_rows, 0),
            (over_c(far_rows), 1),
        ]

    def four_of_plane(share):
        both = lax.ppermute(share, ("y", "x"), DIAGONAL)
        return [share, lax.ppermute(share, "x", FLIP2), lax.ppermute(share, "y", FLIP2), both]

    near = over_c(weights)
    share = far_share(0)
    close, away = pack(place, after(inputs, share), frames)
    share = over_h(share)
    away = over_h(away)
    other_close = swap_half(close)
    up_close, up_away = pack(place, after(grad_out, close), frames, waits=True)
    share = after(share, up_close, valid, near)
    pieces = four_of_plane(share)
    away = after(away, pieces[1:], other_close)
    half_weights = [[weights, near, *pieces, *map(over_c, after(pieces, away))]]
    own = four_of(after(close, away), away)
    other_away = swap_half(away)
    others = [(other_close, 0), (over_c(other_close), 1)]
    params = jnp.stack([gains, shifts + biases, decays], axis=1)
    own_params = params.reshape(LAYERS * 3 * width // LANES, LANES)
    params = None

    def gather(array, axes):
        return lax.all_gather(array, axes, tiled=True)

    weight = half_weights[0]
    early = jnp.concatenate([own_blocks, other_blocks[:2]])
    z, own_flat = project(place, frames, own + others, early, weight, 0, flat=own)
    others += [(other_away, 0), (over_c(after(other_away, z)), 1)]
    z, stats, other_flat = project(
        place,
        frames,
        others[2:],
        other_blocks[2:],
        weight,
        0,
        z,
        valid,
        params=own_params,
        flat=others,
    )
    z = [z]
    stats = gather(stats, ("h", "c"))
    share = over_c(lax.ppermute(after(far_share(1), stats), ("h", "c"), DIAGONAL))
    stats = gather(stats, ("y", "x"))
    x, states, slopes, params = recur(0, place, gate, z, stats, None, valid, own_flat, False)
    own_near, other_near = over_c(after(own_flat, z[0])), over_c(after(other_flat, z[0]))
    x_near = over_c(x)
    own_split = prepare(place, after(own_flat, x_near), own_near)
    other_split = prepare(place, after(other_flat, x_near), other_near)
    saved = [(own_split, other_split, z, stats, states, slopes)]

    pieces = four_of_plane(after(share, slopes, own_near, other_near))
    near = [weights, near]
    other = swap_half(x)
    x_own = after(x, own_split[0], other_split[0])
    z, *_ = project(place, frames, [(x_own, None)], own_blocks, near, 1)
    own_split = prepare(place, after(x, z), x_near)
    far = [*pieces, *map(over_c, after(pieces, own_split[0]))]
    up_away = over_h(after(up_away, other, own_split[0]))
    half_weights.append(near + far)
    z, stats = project(place, frames, [(other, None)], other_blocks, near, 1, z, valid)
    both = jnp.concatenate([own_blocks, other_blocks])
    z_far, stats = project(
        place,
        frames,
        [(x, None), (other, None)],
        both,
        far,
        1,
        None,
        valid,
        stats,
    )
    z = [z, z_far]
    stats = gather(gather(stats, ("y", "x")), ("h", "c"))
    upstream = four_of(up_close, after(up_away, stats))
    *output, states, slopes = recur(1, place, gate, z, stats, params, valid, x, True)
    other_near = over_c(after(other, slopes))
    saved.append((own_split, (other, other_near), z, stats, states, slopes))
    diagonal = over_c(over_h(output[3]))

    ups = upstream
    results = [None] * LAYERS
    for layer in range(LAYERS - 1, -1, -1):
        own_split, other_split, z, stats, states, slopes = saved[layer]
        weight = half_weights[layer]
        grad_pre, sums = back(layer, place, gate, z, stats, params, ups, states, slopes)
        sums = gather(sums, ("y", "x"))
        if layer == 0:
            come[0] = after(come[0], sums, away, output[1][0])
            later, go = step_of((in_hbm(stay[0]), come[0]), (in_hbm(stay[1]), come[1]))
            sums = after(sums, later)
            go = over_second(go)
        sums = gather(sums, ("h", "c"))
        grad_z, leaving, *terms, sums = norm_back(
            other_columns, place, grad_pre, z, params, valid, stats, sums, weight, layer,
            layer == 0,
        )
        leaving = over_c(leaving)
        if layer > 0:
            received = [swap_half(terms[0])]
            other_split = prepare(place, *after(other_split, grad_z))
            leaving = after(leaving, diagonal, other_split[0])
        else:
            received = [None, swap_half(terms[1])]
            later, go = step_of((later, after(go, grad_z)), hbm_outs=(0,))
            leaving = after(leaving, later)
            go = lax.ppermute(go, ("h", "c"), DIAGONAL)
            later = (later, go)
        *first, g_high, g_low = weight_rows(0, place, (grad_z, leaving), own_split, width)
        turned = (g_high, g_low)
        come = [plane_swap(first[1], 0)]
        if layer == 0:
            received[0] = swap_half(after(terms[0], received[1]))
        second = weight_rows(1, place, turned, other_split, width)
        come.append(plane_swap(second[1], 0))
        stay = (first[0], second[0])
        kept = own_terms(own_columns, place, after(grad_z, second[0]), ups, weight, layer)
        if layer > 0:
            away = over_h(after(output[2], kept))
            output = [(a, 0) for a in (output[0], over_c(output[1]), away, diagonal)]
        ups = [(kept, None)] + [(r, None) for r in received]
        results[layer] = lax.dynamic_index_in_dim(
            sums.reshape(3, 4, width), clip, axis=1, keepdims=False
        )

    sums = jnp.stack(results)
    sums = [sums[:, 0], sums[:, 1], sums[:, 2]]
    aways = merge(kept, 1, received[1], apart=True)
    later = (in_hbm(later[0]), over_c(after(later[1], aways[0])))
    come[0] = after(come[0], sums, later[1])
    far_near = over_c(lax.ppermute(aways[0], ("h", "c"), DIAGONAL))
    near_sum, far_sum, near_go, far_go = step_of(
        (in_hbm(stay[0]), come[0]), (in_hbm(stay[1]), come[1]), cut=2
    )
    near_go, far_go = over_second(near_go), over_second(far_go)
    (go,) = step_of((far_sum, after(far_go, far_near)), cut=0)
    (later,) = step_of(later, cut=0)
    later = after(later, go)
    go = over_h(go)
    later = plane_gather(later)
    (total,) = step_of((near_sum, near_go), cut=0)
    output = unpack(place, [(after(array, total), i) for array, i in output], frames, waited=True)
    close = merge(kept, 0, after(received[0], output))
    far = over_c(over_h(after(aways[1], go)))
    (share,) = step_of((total, after(go, close, *later[1:])), cut=0)
    grad_weights = assemble(place, after(later, share), 1)
    gathered = plane_gather(share, grad_weights)
    grad_in = [(close, 0), (over_c(close[frames:]), 0), (far_near, 0), (far, 0)]
    grad_in = unpack(place, grad_in, frames)
    grad_weights = assemble(place, after(gathered, grad_in), 0, grad_weights)
    return (output, grad_in, grad_weights, *sums, sums[1])


def gelu_slope(value):
    return (
        0.5 * (1.0 + jax.scipy.special.erf(value / ROOT_TWO))
        + value * jnp.exp(-0.5 * value * value) / ROOT_TWO_PI
    )


def recur_step(decay, state, inputs):
    drive_t, valid_t = inputs
    pre = drive_t + decay * state
    state = state + valid_t * (jax.nn.gelu(pre, approximate=False) - state)
    return (state, state)


def back_step(decay, carry, inputs):
    upstream_t, valid_t, pre_t = inputs
    total = upstream_t + carry
    grad_pre = total * valid_t * gelu_slope(pre_t)
    carry = total * (1.0 - valid_t) + grad_pre * decay
    return (carry, grad_pre)


def add_piece(weight, piece):
    return jnp.dot(weight, piece, precision=HIGH, preferred_element_type=jnp.float32)


def weight_columns(grad_pre_norm, piece):
    return jnp.einsum("jf,kf->jk", grad_pre_norm, piece, precision=HIGH)


def split_features(inputs, weights, gains, shifts, decays, biases, lengths, frame_mask, grad_out):
    width, slots = inputs.shape
    clips, frames_len = frame_mask.shape
    frames = jnp.arange(frames_len, dtype=jnp.int32)
    valid_grid = (
        (frames[None, :] < lengths[:, None]) & ((frame_mask == 1) | (frames[None, :] == 0))
    ).astype(jnp.float32)
    valid = valid_grid.reshape(-1)
    valid_row = valid[None, :]
    valid_time = jnp.broadcast_to(valid_grid.T[:, :, None], (frames_len, clips, width)).reshape(
        frames_len, clips * width
    )
    count_local = jnp.sum(valid)

    def to_time(array):
        return jnp.transpose(array.reshape(width, clips, frames_len), (2, 1, 0)).reshape(
            frames_len, clips * width
        )

    def from_time(array):
        return jnp.transpose(array.reshape(frames_len, clips, width), (2, 1, 0)).reshape(
            width, slots
        )

    layer_in = inputs
    saved = []
    for layer_no in range(LAYERS):
        weight = weights[layer_no]
        gathered = lax.all_gather(layer_in, "neuron", axis=0, tiled=True)
        pre_norm = add_piece(weight, gathered)
        first_sum, count = lax.psum((jnp.sum(valid_row * pre_norm, axis=1), count_local), "batch")
        mean = first_sum / count
        centered = pre_norm - mean[:, None]
        var = lax.psum(jnp.sum(valid_row * centered * centered, axis=1), "batch") / count
        inv_std = lax.rsqrt(var + EPS)
        zhat = (pre_norm - mean[:, None]) * inv_std[:, None]
        drive = gains[layer_no][:, None] * zhat + (shifts[layer_no] + biases[layer_no])[:, None]
        drive_time = to_time(drive)
        decay_wide = jnp.tile(decays[layer_no], clips)
        start_state = jnp.zeros((clips * width,), jnp.float32)
        _, states = lax.scan(
            partial(recur_step, decay_wide), start_state, (drive_time, valid_time), unroll=8
        )
        saved.append((gathered, zhat, inv_std, drive_time, states, count))
        layer_in = layer_in + valid_row * from_time(states)
    upstream = grad_out
    grad_parts = [None] * LAYERS
    for layer_no in range(LAYERS - 1, -1, -1):
        gathered, zhat, inv_std, drive_time, states, count = saved[layer_no]
        decay_wide = jnp.tile(decays[layer_no], clips)
        gain = gains[layer_no]
        previous = jnp.concatenate([jnp.zeros_like(states[:1]), states[:-1]], axis=0)
        pre_time = drive_time + decay_wide[None, :] * previous
        grad_state = to_time(valid_row * upstream)
        start_carry = jnp.zeros((clips * width,), jnp.float32)
        _, grad_pre_time = lax.scan(
            partial(back_step, decay_wide),
            start_carry,
            (grad_state, valid_time, pre_time),
            reverse=True,
            unroll=8,
        )
        decay_local = jnp.sum(
            jnp.sum(grad_pre_time * previous, axis=0).reshape(clips, width), axis=0
        )
        grad_pre = from_time(grad_pre_time)
        gain_local = jnp.sum(grad_pre * zhat, axis=1)
        shift_local = jnp.sum(grad_pre, axis=1)
        grad_gain, grad_shift, grad_decay = lax.psum(
            (gain_local, shift_local, decay_local), "batch"
        )
        grad_pre_norm = (gain * inv_std)[:, None] * (
            grad_pre - valid_row * (grad_shift[:, None] + zhat * grad_gain[:, None]) / count
        )
        weight_local = weight_columns(grad_pre_norm, gathered)
        input_terms = jnp.einsum("jk,jf->kf", weights[layer_no], grad_pre_norm, precision=HIGH)
        input_grad = lax.psum_scatter(input_terms, "neuron", scatter_dimension=0, tiled=True)
        grad_weight = lax.psum(weight_local, "batch")
        upstream = upstream + input_grad
        grad_parts[layer_no] = (grad_weight, grad_gain, grad_shift, grad_decay)
    grad_weights = jnp.stack([grad_parts[layer_no][0] for layer_no in range(LAYERS)])
    grad_gains = jnp.stack([grad_parts[layer_no][1] for layer_no in range(LAYERS)])
    grad_shifts = jnp.stack([grad_parts[layer_no][2] for layer_no in range(LAYERS)])
    grad_decays = jnp.stack([grad_parts[layer_no][3] for layer_no in range(LAYERS)])
    return (layer_in, upstream, grad_weights, grad_gains, grad_shifts, grad_decays, grad_shifts)


def solution(mesh):
    if (mesh.shape["batch"], mesh.shape["neuron"]) == (4, 8):
        cut = Mesh(mesh.devices.reshape(2, 2, 2, 2, 2), ("y", "x", "h", "l", "c"))
        batch, neuron, body = ("y", "x"), ("h", "l", "c"), half_features
    else:
        cut, batch, neuron, body = mesh, "batch", "neuron", split_features
    in_specs = (
        P(neuron, batch),
        P(None, neuron, None),
        P(None, neuron),
        P(None, neuron),
        P(None, neuron),
        P(None, neuron),
        P(batch),
        P(batch, None),
        P(neuron, batch),
    )
    out_specs = (
        P(neuron, batch),
        P(neuron, batch),
        P(None, neuron, None),
        P(None, neuron),
        P(None, neuron),
        P(None, neuron),
        P(None, neuron),
    )
    return jax.shard_map(
        body, mesh=cut, in_specs=in_specs, out_specs=out_specs, check_vma=False
    )
```

```python
from functools import partial
import math

import jax
import jax.numpy as jnp
from jax import lax
from jax.experimental import pallas as pl
from jax.experimental.pallas import tpu as pltpu
from jax.sharding import Mesh, PartitionSpec as P

LAYERS = 2
EPS = 1e-05
HIGH = lax.Precision.HIGHEST
ROOT_TWO = math.sqrt(2.0)
ROOT_TWO_PI = math.sqrt(2.0 * math.pi)
F32 = jnp.float32
BF16 = jnp.bfloat16
LANES = 128
VMEM_LIMIT = 24 * 1024 * 1024
SMEM_SPEC = pl.BlockSpec(memory_space=pltpu.SMEM)
VMEM_SPEC = pl.BlockSpec(memory_space=pltpu.VMEM)


FLIP2 = [(0, 1), (1, 0)]
DIAGONAL = [(0, 3), (1, 2), (2, 1), (3, 0)]


def swap_half(array):
    return lax.ppermute(array, "l", FLIP2)


def after(value, *others):
    return lax.optimization_barrier((value, others))[0]


def split(value):
    high = value.astype(BF16)
    return high, (value - high.astype(F32)).astype(BF16)


def dot(a, b, dims):
    return lax.dot_general(a, b, (dims, ((), ())), preferred_element_type=F32)


NT = ((1,), (1,))
NN = ((1,), (0,))


def in_hbm(array):
    return pltpu.with_memory_space_constraint(array, pltpu.HBM)


def call(body, out_shape, hbm_outs=(), **kwargs):
    if hbm_outs:
        out_shape = [
            pltpu.HBM(a.shape, a.dtype) if i in hbm_outs else a for i, a in enumerate(out_shape)
        ]
    return pl.pallas_call(
        body,
        out_shape=out_shape,
        compiler_params=pltpu.CompilerParams(vmem_limit_bytes=VMEM_LIMIT),
        **kwargs,
    )


def cost(flops, byte_count):
    return pl.CostEstimate(flops=int(flops) // 64, bytes_accessed=int(byte_count) // 64, transcendentals=0)


def pack_body(frames, place_ref, in_ref, near_ref, far_ref, turned):
    slots = in_ref.shape[1]
    for start in range(0, slots, LANES):
        turned[start : start + LANES, :] = in_ref[:, start : start + LANES].T
    for rel in range(4):
        first = pl.multiple_of(place_ref[rel] * frames, 8)
        out = (near_ref, far_ref)[rel // 2]
        out[(rel % 2) * frames : (rel % 2 + 1) * frames, :] = turned[pl.ds(first, frames), :]


def pack(place, array, frames, waits=False):
    width, slots = array.shape
    out = jax.ShapeDtypeStruct((2 * frames, width), F32)
    return call(
        partial(pack_body, frames),
        grid=(1,),
        out_shape=[out, out],
        in_specs=[SMEM_SPEC, pl.BlockSpec((width, slots), lambda i: (0, 0))],
        out_specs=[pl.BlockSpec(out.shape, lambda i: (0, 0))] * 2,
        scratch_shapes=[pltpu.VMEM((slots, width), F32)],
        hbm_outs=(0, 1) if waits else (),
        cost_estimate=cost(0, 8 * width * slots),
        name="pack",
    )(place, in_hbm(array))


def part_spec(part, frames):
    array, i = part
    if i is None:
        return pl.BlockSpec(array.shape, lambda *_: (0,) * array.ndim)
    return pl.BlockSpec((frames, array.shape[1]), lambda *_: (i, 0))


def arrays_of(parts):
    return [array for array, _ in parts]


def unpack_body(frames, place_ref, *refs):
    ins, out_ref, turned = refs[:4], refs[4], refs[5]
    slots = out_ref.shape[1]
    for rel in range(4):
        first = pl.multiple_of(place_ref[rel] * frames, 8)
        turned[pl.ds(first, frames), :] = ins[rel][...]
    for start in range(0, slots, LANES):
        out_ref[:, start : start + LANES] = turned[start : start + LANES, :].T


def unpack(place, parts, frames, waited=False):
    width = parts[0][0].shape[1]
    slots = 4 * frames
    return call(
        partial(unpack_body, frames),
        grid=(1,),
        out_shape=jax.ShapeDtypeStruct((width, slots), F32),
        in_specs=[SMEM_SPEC] + [part_spec(part, frames) for part in parts],
        out_specs=pl.BlockSpec((width, slots), lambda i: (0, 0)),
        scratch_shapes=[pltpu.VMEM((slots, width), F32)],
        cost_estimate=cost(0, 8 * width * slots),
        name="unpack",
    )(place, *[in_hbm(a) if waited else a for a in arrays_of(parts)])


def merge_body(kept_ref, come_ref, *outs):
    frames, columns = kept_ref.shape
    width = columns // 2
    for i in range(2):
        some = slice(i * width, (i + 1) * width)
        if len(outs) > 1:
            outs[i][...] = kept_ref[:, some] + come_ref[:, some]
            continue
        (out_ref,) = outs
        out_ref[i * frames : (i + 1) * frames, :] = kept_ref[:, some] + come_ref[:, some]


def merge(kept, half, come, apart=False):
    frames, columns = come.shape
    rows, n = (frames, 2) if apart else (2 * frames, 1)
    outs = call(
        merge_body,
        hbm_outs=(0, 1) if apart else (),
        grid=(1,),
        out_shape=[jax.ShapeDtypeStruct((rows, columns // 2), F32)] * n,
        in_specs=[
            pl.BlockSpec((frames, columns), lambda i: (0, half)),
            pl.BlockSpec((frames, columns), lambda i: (0, 0)),
        ],
        out_specs=[pl.BlockSpec((rows, columns // 2), lambda i: (0, 0))] * n,
        cost_estimate=cost(0, 12 * frames * columns),
        name="merge",
    )(kept, come)
    return outs if apart else outs[0]


def project_body(n_parts, n_flat, spots, n_weights, first, with_acc, with_stats, with_params, cols_ref, place_ref, *refs):
    del cols_ref

    def take(n):
        nonlocal refs
        some, refs = refs[:n], refs[n:]
        return some

    parts, flat_parts, weights = take(n_parts), take(n_flat), take(n_weights)
    acc, valid, stats_in, params = take(with_acc), take(with_stats > 0), take(with_stats > 1), take(with_params)
    (out_ref,) = take(1)
    stats, flat = take(with_stats > 0), take(n_flat > 0)
    x_high, x_low, far_ref = refs
    step = pl.program_id(0)
    width = x_high.shape[2]

    @pl.when(step == 0)
    def _():
        for block, part in zip(spots, parts):
            for start in range(0, part.shape[1], width):
                high, low = split(part[:, start : start + width])
                x_high[block + start // width] = high
                x_low[block + start // width] = low
        column = 0
        for part in flat_parts:
            flat[0][:, column : column + part.shape[1]] = part[...]
            column += part.shape[1]
        if with_acc:
            out_ref[...] = acc[0][...]
        else:
            out_ref[...] = jnp.zeros_like(out_ref)

    stacked = jnp.concatenate([x_high[step], x_low[step], x_high[step]], axis=1)
    for block, weight in enumerate(weight_blocks(place_ref, weights, far_ref)):
        w_high, w_low = split(weight)
        columns = slice(block * width, (block + 1) * width)
        out_ref[:, columns] += dot(stacked, jnp.concatenate([w_high, w_high, w_low], axis=1), NT)

    if with_stats:
        (stats_ref,) = stats

        @pl.when(step == pl.num_programs(0) - 1)
        def _():
            if stats_in:
                stats_ref[...] = stats_in[0][...]
            own = jnp.sum(valid[0][...], axis=0, keepdims=True)
            per = width // LANES
            for row in range(out_ref.shape[1] // LANES):
                z = out_ref[:, row * LANES : (row + 1) * LANES]
                total = jnp.sum(valid[0][...] * z, axis=0, keepdims=True)
                centred = valid[0][...] * (z - total / own)
                squares = jnp.sum(centred * centred, axis=0, keepdims=True)
                at = place_ref[first + row // per] * per + row % per
                stats_ref[0, pl.ds(at, 1), :] = total
                stats_ref[1, pl.ds(at, 1), :] = squares
                stats_ref[2, pl.ds(at, 1), :] = own
            if with_params:
                rest = params[0].shape[0] - 8
                stats_ref[3] = params[0][:8, :]
                stats_ref[4] = jnp.zeros_like(stats_ref[4])
                stats_ref[4, :rest, :] = params[0][8:, :]


def weight_specs(weights, layer, pairs=2):
    specs = []
    for weight in weights:
        if weight.ndim == 3:
            shape = (1, weight.shape[1], pairs * weight.shape[1])
            specs.append(pl.BlockSpec(shape, lambda s, cols, *_: (layer, 0, cols[s])))
        else:
            shape = (weight.shape[0], pairs * 4 * weight.shape[0])
            specs.append(pl.BlockSpec(shape, lambda s, cols, *_: (0, cols[s])))
    return specs


def far_scratch(width, pairs=2):
    return pltpu.VMEM((2, width, pairs * width), F32)


def weight_blocks(place_ref, refs, far_ref):
    near = [ref[0] for ref in refs if len(ref.shape) == 3]
    pieces = [ref for ref in refs if len(ref.shape) == 2]
    far = []
    for i in range(len(pieces) // 4):
        for rel, piece in enumerate(pieces[4 * i : 4 * i + 4]):
            rows = piece.shape[0]
            row = 2 * (place_ref[4] ^ (rel // 2)) + (place_ref[5] ^ (rel % 2))
            far_ref[i, pl.ds(pl.multiple_of(row * rows, rows), rows), :] = piece[...]
        far.append(far_ref[i])
    return near + far


def project(
    place, frames, parts, blocks, weights, layer, acc=None, valid=None, stats=None, params=None, flat=()
):
    near = weights[0].ndim == 3
    units = sum(1 if w.ndim == 3 else 0.25 for w in weights)
    width = weights[0].shape[1] if near else 4 * weights[0].shape[0]
    n = blocks.shape[0]
    spots, block = [], 0
    for array, _ in parts:
        spots.append(block)
        block += array.shape[1] // width
    full = pl.BlockSpec(memory_space=pltpu.VMEM)
    in_specs = [part_spec(part, frames) for part in (*parts, *flat)]
    in_specs += weight_specs(weights, layer, 1)
    operands = arrays_of(parts) + arrays_of(flat) + [in_hbm(w) for w in weights]
    array = jax.ShapeDtypeStruct((frames, int(units) * width), F32)
    array_spec = pl.BlockSpec(array.shape, lambda s, cols, place: (0, 0))
    out_shape, out_specs = [array], [array_spec]
    if acc is not None:
        in_specs.append(array_spec)
        operands.append(in_hbm(acc))
    if valid is not None:
        in_specs.append(full)
        operands.append(valid)
        shape = (3 if params is None else 5, 4 * width // LANES, LANES)
        out_shape.append(jax.ShapeDtypeStruct(shape, F32))
        out_specs.append(pl.BlockSpec(shape, lambda s, cols, place: (0, 0, 0)))
    for extra in (stats, params):
        if extra is not None:
            in_specs.append(full)
            operands.append(extra)
    if flat:
        out_shape.append(jax.ShapeDtypeStruct((frames, 4 * width), F32))
        out_specs.append(pl.BlockSpec((frames, 4 * width), lambda s, cols, place: (0, 0)))
    return call(
        partial(
            project_body,
            len(parts),
            len(flat),
            spots,
            len(weights),
            0 if near else 2,
            acc is not None,
            (valid is not None) + (stats is not None),
            params is not None,
        ),
        grid_spec=pltpu.PrefetchScalarGridSpec(
            num_scalar_prefetch=2,
            grid=(n,),
            in_specs=in_specs,
            out_specs=out_specs,
            scratch_shapes=[pltpu.VMEM((n, frames, width), BF16)] * 2 + [far_scratch(width, 1)],
        ),
        out_shape=out_shape,
        hbm_outs=(0, len(out_shape) - 1) if flat else (0,),
        cost_estimate=cost(6 * frames * n * width * units * width, 4 * n * width * units * width),
        name="project",
    )(blocks, place, *operands)


def to_relative(place_ref, spread, rows_ref, value, slot):
    per = value.shape[0] // 4
    spread[...] = value
    for rel in range(4):
        first = place_ref[rel] * per
        for row in range(per):
            rows_ref[slot, rel * per + row : rel * per + row + 1, :] = spread[
                pl.ds(first + row, 1), :
            ]


def tree(values):
    while len(values) > 1:
        values = [a + b for a, b in zip(values[::2], values[1::2])]
    return values[0]


def gathered(ref, slot):
    return [ref[i] for i in range(slot, ref.shape[0], ref.shape[0] // 16)]


def norm_terms(stats_ref):
    each = [gathered(stats_ref, slot) for slot in range(3)]
    totals, squares, owns = each
    count = tree(owns)
    mean = tree(totals) / count
    away = [total / own - mean for total, own in zip(totals, owns)]
    spread = tree([s + n * a * a for s, n, a in zip(squares, owns, away)])
    return count, mean, lax.rsqrt(spread / count + EPS)


CHUNKS = 4


def columns_of(refs, row):
    for ref in refs:
        if row * LANES < ref.shape[1]:
            return ref[:, row * LANES : (row + 1) * LANES]
        row -= ref.shape[1] // LANES


def recur_body(n_z, last, layer, spread_params, place_ref, gate_ref, *refs):
    z_refs, refs = refs[:n_z], refs[n_z:]
    (stats_ref, params_ref, valid_ref, x_ref), refs = refs[:4], refs[4:]
    outs, refs = refs[: 1 + 3 * last], refs[1 + 3 * last :]
    if spread_params:
        state_ref, slope_ref, params_out, rows, spread, held, drive_s, state_s, slope_s = refs
    else:
        state_ref, slope_ref, rows, spread, held, drive_s, state_s, slope_s = refs
    frames, features = x_ref.shape
    blocks = features // LANES
    per = blocks // 4
    chunk = pl.program_id(0)

    @pl.when(chunk == 0)
    def _():
        if spread_params:
            for rel in range(4):
                first = place_ref[rel] * (stats_ref.shape[0] // 16) + 3
                for row in range(LAYERS * 3 * per):
                    at = rel * per + row % per
                    params_out[row // per, at : at + 1, :] = stats_ref[
                        first + row // 8, row % 8 : row % 8 + 1, :
                    ]
            params = [params_out[3 * layer + i] for i in range(3)]
        else:
            params = [params_ref[3 * layer + i] for i in range(3)]
        _, mean, inv_std = norm_terms(stats_ref)
        to_relative(place_ref, spread, rows, mean, 0)
        to_relative(place_ref, spread, rows, inv_std, 1)
        rows[1] = rows[1] * params[0]
        rows[2] = params[1]
        rows[3] = params[2]
        held[...] = jnp.zeros_like(held)

    for row in range(blocks):
        drive_s[row * frames : (row + 1) * frames, :] = (
            columns_of(z_refs, row) - rows[0, row : row + 1, :]
        ) * rows[1, row : row + 1, :] + rows[2, row : row + 1, :]
    decay = rows[3]

    def step(t, state):
        at = pl.ds(t, blocks, stride=frames)
        pre = drive_s[at, :] + decay * state
        half = 0.5 + 0.5 * lax.erf(pre * (1.0 / ROOT_TWO))
        gate = gate_ref[chunk * frames + t] > 0.0
        slope = half + pre * jnp.exp(-0.5 * pre * pre) * (1.0 / ROOT_TWO_PI)
        state = jnp.where(gate, pre * half, state)
        state_s[at, :] = state
        slope_s[at, :] = jnp.where(gate, slope, 0.0)
        return state

    held[...] = lax.fori_loop(0, frames, step, held[...], unroll=8)
    valid = valid_ref[...]
    for row in range(blocks):
        lanes = slice(row * LANES, (row + 1) * LANES)
        state = state_s[row * frames : (row + 1) * frames, :]
        state_ref[:, lanes] = state
        slope_ref[:, lanes] = slope_s[row * frames : (row + 1) * frames, :]
        value = x_ref[:, lanes] + valid * state
        out, at = (outs[row // per], row % per) if last else (outs[0], row)
        out[:, at * LANES : (at + 1) * LANES] = value


def recur(layer, place, gate, z, stats, params, valid, x, last):
    frames, features = x.shape
    blocks = features // LANES
    some = frames // CHUNKS
    whole = lambda array: pl.BlockSpec(array.shape, lambda i: (0,) * array.ndim)
    by_chunk = lambda array: pl.BlockSpec((some, array.shape[1]), lambda i: (i, 0))
    full = jax.ShapeDtypeStruct((frames, features), F32)
    piece = jax.ShapeDtypeStruct((frames, features // 4), F32)
    out_shape = [piece] * 4 if last else [full]
    out_shape += [full, full]
    out_specs = [by_chunk(a) for a in out_shape]
    spread_params = params is None
    if spread_params:
        out_shape.append(jax.ShapeDtypeStruct((3 * LAYERS, blocks, LANES), F32))
        out_specs.append(whole(out_shape[-1]))
        params = valid
    return call(
        partial(recur_body, len(z), last, layer, spread_params),
        grid=(CHUNKS,),
        in_specs=[SMEM_SPEC, SMEM_SPEC]
        + [by_chunk(a) for a in z]
        + [whole(a) for a in (stats, params)]
        + [by_chunk(a) for a in (valid, x)],
        out_specs=out_specs,
        out_shape=out_shape,
        hbm_outs=tuple(range(len(out_shape) - spread_params)) if last else (1, 2),
        scratch_shapes=[
            pltpu.VMEM((4, blocks, LANES), F32),
            pltpu.VMEM((blocks, LANES), F32),
            pltpu.VMEM((blocks, LANES), F32),
        ]
        + [pltpu.VMEM((blocks * some, LANES), F32)] * 3,
        cost_estimate=cost(100 * frames * features, 20 * frames * features),
        name="recur",
    )(place, gate, *[in_hbm(a) for a in z], stats, params, valid, in_hbm(x))


def back_body(n_z, n_ups, spots, layer, place_ref, gate_ref, *refs):
    z_refs, refs = refs[:n_z], refs[n_z:]
    (stats_ref, params_ref), refs = refs[:2], refs[2:]
    ups, (state_ref, slope_ref), refs = refs[:n_ups], refs[n_ups : n_ups + 2], refs[n_ups + 2 :]
    grad_ref, sums_ref, rows, spread, held, up_s, state_s, slope_s = refs
    frames, features = state_ref.shape
    blocks = features // LANES
    per = blocks // 4
    tall = frames + 8
    step_no = pl.program_id(0)
    chunk = pl.num_programs(0) - 1 - step_no

    @pl.when(step_no == 0)
    def _():
        _, mean, inv_std = norm_terms(stats_ref)
        to_relative(place_ref, spread, rows, mean, 0)
        to_relative(place_ref, spread, rows, inv_std, 1)
        held[...] = jnp.zeros_like(held)

    for row in range(blocks):
        lanes = slice(row * LANES, (row + 1) * LANES)
        base = row * frames
        up = None
        for (_, column), part in zip(spots, ups):
            if column <= row * LANES < column + part.shape[1]:
                value = part[:, row * LANES - column : (row + 1) * LANES - column]
                up = value if up is None else up + value
        up_s[base : base + frames, :] = up
        state_s[row * tall : row * tall + 8, :] = jnp.zeros((8, LANES), F32)
        state_s[row * tall + 8 : (row + 1) * tall, :] = state_ref[:, lanes]
        slope_s[base : base + frames, :] = slope_ref[:, lanes]
    decay = params_ref[3 * layer + 2]

    def step(i, carry):
        t = frames - 1 - i
        at = pl.ds(t, blocks, stride=frames)
        slope = slope_s[at, :]
        gate = gate_ref[chunk * frames + t]
        total = gate * up_s[at, :] + carry
        up_s[at, :] = total * slope
        return total * (slope * decay + (1.0 - gate))

    held[0] = lax.fori_loop(0, frames, step, held[0], unroll=8)
    held[4] += held[1] * state_s[pl.ds(tall - 1, blocks, stride=tall), :]
    held[1] = up_s[pl.ds(0, blocks, stride=frames), :]
    for row in range(blocks):
        lanes = slice(row * LANES, (row + 1) * LANES)
        grad = up_s[row * frames : (row + 1) * frames, :]
        grad_ref[:, lanes] = grad
        zhat = (columns_of(z_refs, row) - rows[0, row : row + 1, :]) * rows[1, row : row + 1, :]
        before = state_s[row * tall + 7 : row * tall + 7 + frames, :]
        for slot, value in enumerate((grad * zhat, grad, grad * before)):
            held[2 + slot, row : row + 1, :] += jnp.sum(value, axis=0, keepdims=True)

    @pl.when(chunk == 0)
    def _():
        for row in range(blocks):
            at = place_ref[row // per] * per + row % per
            for slot in range(3):
                sums_ref[slot, pl.ds(at, 1), :] = held[2 + slot, row : row + 1, :]


def spots_of_sum(parts, width):
    spots, column = [], 0
    for array, _ in parts:
        spots.append((0, column % (4 * width)))
        column += array.shape[1]
    return spots


def back(layer, place, gate, z, stats, params, ups, states, slopes):
    frames, features = states.shape
    width = features // 4
    blocks = features // LANES
    some = frames // CHUNKS
    whole = lambda array: pl.BlockSpec(array.shape, lambda i: (0,) * array.ndim)

    def by_chunk(array, first=0):
        return pl.BlockSpec(
            (some, array.shape[1]), lambda i: ((first or 0) * CHUNKS + CHUNKS - 1 - i, 0)
        )

    out_shape = [
        jax.ShapeDtypeStruct((frames, features), F32),
        jax.ShapeDtypeStruct((3, blocks, LANES), F32),
    ]
    return call(
        partial(back_body, len(z), len(ups), spots_of_sum(ups, width), layer),
        grid=(CHUNKS,),
        in_specs=[SMEM_SPEC] * 2
        + [by_chunk(a) for a in z]
        + [whole(a) for a in (stats, params)]
        + [by_chunk(*up) for up in ups]
        + [by_chunk(a) for a in (states, slopes)],
        out_specs=[by_chunk(out_shape[0]), whole(out_shape[1])],
        out_shape=out_shape,
        scratch_shapes=[
            pltpu.VMEM((2, blocks, LANES), F32),
            pltpu.VMEM((blocks, LANES), F32),
            pltpu.VMEM((5, blocks, LANES), F32),
            pltpu.VMEM((blocks * some, LANES), F32),
            pltpu.VMEM((blocks * (some + 8), LANES), F32),
            pltpu.VMEM((blocks * some, LANES), F32),
        ],
        cost_estimate=cost(30 * frames * features, 20 * frames * features),
        name="back",
    )(
        place,
        gate,
        *[in_hbm(a) for a in z],
        stats,
        params,
        *arrays_of(ups),
        in_hbm(states),
        in_hbm(slopes),
    )


def input_terms(high_s, low_s, weights):
    left, right = [], []
    for block, weight in enumerate(weights):
        w_high, w_low = split(weight)
        left += [high_s[block], low_s[block], high_s[block]]
        right += [w_high, w_high, w_low]
    return dot(jnp.concatenate(left, axis=1), jnp.concatenate(right, axis=0), NN)


def norm_back_body(n_z, split_terms, layer, cols_ref, place_ref, grad_ref, *refs):
    del cols_ref
    z_refs, refs = refs[:n_z], refs[n_z:]
    params_ref, valid_ref, stats_ref, sums_ref, *refs = refs
    weights, refs = refs[:10], refs[10:]
    if split_terms:
        out_ref, leave_ref, near_term_ref, far_term_ref, sums_out_ref, *refs = refs
        term_refs, starts = (far_term_ref, near_term_ref), (0, 0)
    else:
        out_ref, leave_ref, term_ref, sums_out_ref, *refs = refs
        term_refs, starts = (term_ref, term_ref), (2 * grad_ref.shape[1] // 4, 0)
    rows, spread, high_s, low_s, far_ref = refs
    blocks = grad_ref.shape[1] // LANES
    width = high_s.shape[2]
    per = width // LANES

    @pl.when(pl.program_id(0) == 0)
    def _():
        count, mean, inv_std = norm_terms(stats_ref)
        to_relative(place_ref, spread, rows, mean, 0)
        to_relative(place_ref, spread, rows, inv_std, 1)
        rows[2] = rows[1] * params_ref[3 * layer]
        sums = [tree(gathered(sums_ref, slot)) for slot in range(3)]
        for slot in range(3):
            sums_out_ref[slot] = sums[slot]
        to_relative(place_ref, spread, rows, sums[0] / count, 3)
        to_relative(place_ref, spread, rows, sums[1] / count, 4)
        valid = valid_ref[...]
        for row in range(blocks):
            lanes = slice(row * LANES, (row + 1) * LANES)
            one = lambda slot: rows[slot, row : row + 1, :]
            zhat = (columns_of(z_refs, row) - one(0)) * one(1)
            value = one(2) * (grad_ref[:, lanes] - valid * (one(4) + zhat * one(3)))
            out_ref[:, lanes] = value
            if (row // per) % 2:
                at = (row // per // 2) * width + (row % per) * LANES
                leave_ref[:, at : at + LANES] = value
            high, low = split(value)
            inner = slice((row % per) * LANES, (row % per + 1) * LANES)
            high_s[row // per, :, inner] = high
            low_s[row // per, :, inner] = low

    value = input_terms(high_s, low_s, weight_blocks(place_ref, weights, far_ref))
    for step, (term_ref, first) in enumerate(zip(term_refs, starts)):

        @pl.when(pl.program_id(0) == step)
        def _():
            for pair in range(2):
                at = pl.multiple_of(((place_ref[0] & 1) ^ pair) * width, width)
                term_ref[:, pl.ds(first + at, width)] = value[
                    :, pair * width : (pair + 1) * width
                ]


def norm_back(columns, place, grad, z, params, valid, stats, sums, weights, layer, split_terms):
    frames, features = grad.shape
    width = features // 4
    blocks = features // LANES
    whole = lambda array: pl.BlockSpec(array.shape, lambda s, cols, place: (0,) * array.ndim)
    operands = [grad, *[in_hbm(a) for a in z], params, valid, stats, sums]
    full = jax.ShapeDtypeStruct((frames, features), F32)
    half = jax.ShapeDtypeStruct((frames, 2 * width), F32)
    terms = [half, half] if split_terms else [full]
    out_shape = [full, half, *terms, jax.ShapeDtypeStruct((3, blocks, LANES), F32)]
    return call(
        partial(norm_back_body, len(z), split_terms, layer),
        grid_spec=pltpu.PrefetchScalarGridSpec(
            num_scalar_prefetch=2,
            grid=(2,),
            in_specs=[whole(a) for a in operands] + weight_specs(weights, layer),
            out_specs=[whole(a) for a in out_shape],
            scratch_shapes=[
                pltpu.VMEM((5, blocks, LANES), F32),
                pltpu.VMEM((blocks, LANES), F32),
                pltpu.VMEM((4, frames, width), BF16),
                pltpu.VMEM((4, frames, width), BF16),
                far_scratch(width),
            ],
        ),
        out_shape=out_shape,
        hbm_outs=(0, 2) if split_terms else (0,),
        cost_estimate=cost(6 * frames * features * features, 4 * features * features),
        name="norm_back",
    )(columns, place, *operands, *[in_hbm(w) for w in weights])


def own_terms_body(n_ups, spots, cols_ref, place_ref, grad_ref, *refs):
    del cols_ref
    ups, refs = refs[:n_ups], refs[n_ups:]
    weights, refs = refs[:10], refs[10:]
    out_ref, high_s, low_s, far_ref = refs
    width = high_s.shape[2]
    step = pl.program_id(0)

    @pl.when(step == 0)
    def _():
        for block in range(4):
            high, low = split(grad_ref[:, block * width : (block + 1) * width])
            high_s[block] = high
            low_s[block] = low

    value = input_terms(high_s, low_s, weight_blocks(place_ref, weights, far_ref))
    for pair in range(2):
        at = pl.multiple_of(((place_ref[0] & 1) ^ pair) * width, width)
        out_ref[:, pl.ds(at, width)] = value[:, pair * width : (pair + 1) * width]
    for half in range(2):

        @pl.when(step == half)
        def _():
            first = 2 * half * width
            for (_, column), up in zip(spots, ups):
                low = max(column, first)
                high = min(column + up.shape[1], first + 2 * width)
                if low < high:
                    out_ref[:, low - first : high - first] += up[:, low - column : high - column]


def own_terms(columns, place, grad, ups, weights, layer):
    frames, features = grad.shape
    width = features // 4
    whole = lambda array: pl.BlockSpec(array.shape, lambda s, cols, place: (0,) * array.ndim)
    step_block = pl.BlockSpec((frames, 2 * width), lambda s, cols, place: (0, s))
    return call(
        partial(own_terms_body, len(ups), spots_of_sum(ups, width)),
        grid_spec=pltpu.PrefetchScalarGridSpec(
            num_scalar_prefetch=2,
            grid=(2,),
            in_specs=[whole(grad)]
            + [part_spec(up, frames) for up in ups]
            + weight_specs(weights, layer),
            out_specs=step_block,
            scratch_shapes=[pltpu.VMEM((4, frames, width), BF16)] * 2 + [far_scratch(width)],
        ),
        out_shape=jax.ShapeDtypeStruct((frames, features), F32),
        cost_estimate=cost(6 * frames * features * features, 4 * features * features),
        name="own_terms",
    )(columns, place, in_hbm(grad), *arrays_of(ups), *[in_hbm(w) for w in weights])


def prepare_body(lists_ref, place_ref, own_ref, near_ref, high_ref, low_ref):
    del lists_ref
    padded = high_ref.shape[0] // 2
    width = high_ref.shape[1] // 2
    for clip, part in enumerate((own_ref, near_ref)):
        rows = part.shape[0]
        for dc in range(2):
            at = pl.multiple_of((place_ref[6] ^ clip ^ dc) * width, width)
            high, low = split(part[:, dc * width : (dc + 1) * width])
            high_ref[clip * padded : clip * padded + rows, pl.ds(at, width)] = high
            low_ref[clip * padded : clip * padded + rows, pl.ds(at, width)] = low
        zeros = jnp.zeros((padded - rows, 2 * width), BF16)
        high_ref[clip * padded + rows : (clip + 1) * padded, :] = zeros
        low_ref[clip * padded + rows : (clip + 1) * padded, :] = zeros


def prepare(place, own, near):
    frames, features = own.shape
    width = features // 4
    padded = -(-frames // LANES) * LANES
    in_spec = pl.BlockSpec((frames, 2 * width), lambda s, *_: (0, s))
    out = jax.ShapeDtypeStruct((2 * padded, features), BF16)
    out_spec = pl.BlockSpec((2 * padded, 2 * width), lambda s, order, place: (0, order[s]))
    order = jnp.stack([place[0] >> 1, 1 - (place[0] >> 1)])
    return call(
        prepare_body,
        grid_spec=pltpu.PrefetchScalarGridSpec(
            num_scalar_prefetch=2,
            grid=(2,),
            in_specs=[in_spec, in_spec],
            out_specs=[out_spec, out_spec],
        ),
        out_shape=[out, out],
        hbm_outs=(0, 1),
        cost_estimate=cost(0, 16 * frames * features),
        name="prepare",
    )(order, place, in_hbm(own), in_hbm(near))


def product(g_high, g_low, x_high, x_low):
    return dot(g_high, x_high, NN) + (dot(g_high, x_low, NN) + dot(g_low, x_high, NN))


def weight_body(turn, place_ref, *refs):
    if turn:
        grad_ref, near_ref, x_high, x_low, kept, sent, g_high, g_low, t_high, t_low = refs

        @pl.when(pl.program_id(0) == 0)
        def _():
            frames, features = grad_ref.shape
            width = features // 4
            rows = width // 4
            padded = t_high.shape[1] // 2
            t_high[...] = jnp.zeros_like(t_high)
            t_low[...] = jnp.zeros_like(t_low)
            for clip in range(2):
                for dh in range(2):
                    if clip == 0:
                        part = grad_ref[:, 2 * dh * width : (2 * dh + 1) * width]
                    else:
                        part = near_ref[:, dh * width : (dh + 1) * width]
                    high, low = split(part.T)
                    at = (
                        slice(dh * width, (dh + 1) * width),
                        slice(clip * padded, clip * padded + frames),
                    )
                    t_high[at] = high
                    t_low[at] = low
            for group in range(8):
                first, second, dh = group // 4, group // 2 % 2, group % 2
                core = place_ref[6]
                y = place_ref[4] ^ (first * core + second * (1 - core))
                x = place_ref[5] ^ (first * (1 - core) + second * core)
                at = pl.multiple_of(dh * width + (2 * y + x) * rows, rows)
                g_high[group * rows : (group + 1) * rows, :] = t_high[pl.ds(at, rows), :]
                g_low[group * rows : (group + 1) * rows, :] = t_low[pl.ds(at, rows), :]

    else:
        g_high, g_low, x_high, x_low, kept, sent = refs
    half = g_high.shape[0] // 2
    value = product(g_high[...], g_low[...], x_high[...], x_low[...])
    kept[...] = value[:half].reshape(kept.shape)
    sent[...] = value[half:].reshape(sent.shape)


def weight_rows(side, place, grads, x_split, width):
    turn = side == 0
    whole = lambda array: pl.BlockSpec(array.shape, lambda s, place: (0,) * array.ndim)
    x_spec = pl.BlockSpec((x_split[0].shape[0], width), lambda s, place: (0, s))
    shape = (2, 2, width // 4, 4 * width)
    out_shape = [jax.ShapeDtypeStruct(shape, F32)] * 2
    out_specs = [pl.BlockSpec(shape[:3] + (width,), lambda s, place: (0, 0, 0, s))] * 2
    scratch = []
    if turn:
        turned = (2 * width, x_split[0].shape[0])
        out_shape += [jax.ShapeDtypeStruct(turned, BF16)] * 2
        out_specs += [whole(out_shape[-1])] * 2
        scratch = [pltpu.VMEM(turned, BF16)] * 2
    return call(
        partial(weight_body, turn),
        grid_spec=pltpu.PrefetchScalarGridSpec(
            num_scalar_prefetch=1,
            grid=(4,),
            in_specs=[whole(a) for a in grads] + [x_spec] * 2,
            out_specs=out_specs,
            scratch_shapes=scratch,
        ),
        out_shape=out_shape,
        hbm_outs=(0,),
        cost_estimate=cost(12 * x_split[0].shape[0] * width * 4 * width, 4 * 8 * width * width),
        name="weight_rows",
    )(place, *([in_hbm(grads[0]), grads[1]] if turn else grads), *[in_hbm(x) for x in x_split])


def step_body(n, widths, cut, *refs):
    ins, outs = refs[: 2 * n], refs[2 * n :]
    starts = [sum(widths[:i]) for i in range(len(widths))]
    column = 0
    for i in range(n):
        total = ins[2 * i][...] + ins[2 * i + 1][...]
        end = column + total.shape[-1]
        for j, (start, columns) in enumerate(zip(starts, widths)):
            low, high = max(start, column), min(start + columns, end)
            if low < high:
                to = (Ellipsis, slice(low - start, high - start))
                piece = total[..., low - column : high - column]
                pieces = [piece]
                for _ in range(cut):
                    pieces = [half[k] for half in pieces for k in range(2)]
                for k, some in enumerate(pieces):
                    outs[len(pieces) * j + k][to] = some
        column = end


def step_of(*pairs, cut=1, widths=None, hbm_outs=()):
    shape = list(pairs[0][0].shape)
    widths = widths or [sum(pair[0].shape[-1] for pair in pairs)]
    outs = []
    for columns in widths:
        shape[-1] = columns
        outs += [jax.ShapeDtypeStruct(tuple(shape[cut:]), F32)] * 2**cut
    whole = lambda array: pl.BlockSpec(array.shape, lambda i: (0,) * array.ndim)
    operands = [array for pair in pairs for array in pair]
    return call(
        partial(step_body, len(pairs), widths, cut),
        grid=(1,),
        in_specs=[whole(a) for a in operands],
        out_specs=[whole(a) for a in outs],
        out_shape=outs,
        hbm_outs=hbm_outs,
        cost_estimate=cost(0, 4 * sum(a.size for a in operands)),
        name="reduction_step",
    )(*operands)


def plane_swap(array, step):
    pairs = []
    for i in range(8):
        over_x = (i % 2 == 0) == (step == 0)
        pairs.append((i, i ^ 2 if over_x else i ^ 4))
    return lax.ppermute(array, ("y", "x", "c"), pairs)


def plane_gather(share, *before):
    first = plane_swap(share, 0)
    second = plane_swap(share, 1)
    return [share, second, first, plane_swap(after(first, second, *before), 1)]


def assemble_body(place_ref, *refs):
    out_ref = refs[-1]
    core = place_ref[6]
    rows, columns = refs[0].shape
    quarter = columns // 4
    for i in range(4):
        first, second = i // 2, i % 2
        y = place_ref[4] ^ (first * core + second * (1 - core))
        x = place_ref[5] ^ (first * (1 - core) + second * core)
        at = pl.multiple_of((2 * y + x) * rows, rows)
        for side in range(2):
            for h in range(2):
                to = pl.multiple_of((2 * h + (place_ref[7] ^ side)) * quarter, quarter)
                some = slice((2 * side + h) * quarter, (2 * side + h + 1) * quarter)
                out_ref[0, pl.ds(at, rows), pl.ds(to, quarter)] = refs[i][:, some]


def assemble(place, pieces, layer, onto=None):
    rows, columns = 4 * pieces[0].shape[0], pieces[0].shape[1]
    aliases, extra, extra_specs = {}, [], []
    if onto is not None:
        aliases, extra = {1 + len(pieces): 0}, [onto]
        extra_specs = [pl.BlockSpec(memory_space=pl.ANY)]
    (out,) = call(
        assemble_body,
        grid=(1,),
        out_shape=[jax.ShapeDtypeStruct((LAYERS, rows, columns), F32)],
        hbm_outs=(0,),
        in_specs=[SMEM_SPEC]
        + [pl.BlockSpec(p.shape, lambda i: (0, 0)) for p in pieces]
        + extra_specs,
        out_specs=[pl.BlockSpec((1, rows, columns), lambda i: (layer, 0, 0))],
        input_output_aliases=aliases,
        cost_estimate=cost(0, 8 * rows * columns),
        name="assemble",
    )(place, *[p if extra else in_hbm(p) for p in pieces], *extra)
    return out


def half_features(inputs, weights, gains, shifts, decays, biases, lengths, frame_mask, grad_out):
    width, slots = inputs.shape
    clips, frames = frame_mask.shape
    depth = weights.shape[2]
    blocks = 4 * width // LANES
    y, x, h, l, c = (lax.axis_index(name) for name in ("y", "x", "h", "l", "c"))
    b = 2 * y + x
    numbers = [2 * (h ^ (rel // 2)) + (c ^ (rel % 2)) for rel in range(4)] + [y, x, c, l]
    place = jnp.stack(numbers).astype(jnp.int32)
    own_blocks, other_blocks = (
        jnp.stack(
            [2 * (2 * (h ^ (rel // 2)) + half) + (c ^ (rel % 2)) for rel in range(4)]
        ).astype(jnp.int32)
        for half in (l, 1 - l)
    )
    own_columns = jnp.stack([2 * h + l, 2 * (1 - h) + l]).astype(jnp.int32)
    other_columns = jnp.stack([2 * (1 - h) + 1 - l, 2 * h + 1 - l]).astype(jnp.int32)
    rows = width // 4

    clip = 2 * h + c
    seen = lax.dynamic_index_in_dim(frame_mask, clip, 0, keepdims=False)
    length = lax.dynamic_index_in_dim(lengths, clip, 0, keepdims=False)
    moments = jnp.arange(frames, dtype=jnp.int32)
    gate = ((moments < length) & ((seen == 1) | (moments == 0))).astype(F32)
    valid = jnp.broadcast_to(gate[:, None], (frames, LANES))

    def far_share(layer):
        return lax.dynamic_slice(weights, (layer, b * rows, 0), (1, rows, depth))[0]

    def over_h(array):
        return lax.ppermute(array, "h", FLIP2)

    def over_c(array):
        return lax.ppermute(array, "c", FLIP2)

    def over_second(array):
        return plane_swap(array, 1)

    def four_of(near_rows, far_rows):
        return [
            (near_rows, 0),
            (over_c(near_rows), 1),
            (far_rows, 0),
            (over_c(far_rows), 1),
        ]

    def four_of_plane(share):
        both = lax.ppermute(share, ("y", "x"), DIAGONAL)
        return [share, lax.ppermute(share, "x", FLIP2), lax.ppermute(share, "y", FLIP2), both]

    near = over_c(weights)
    share = far_share(0)
    close, away = pack(place, after(inputs, share), frames)
    share = over_h(share)
    away = over_h(away)
    other_close = swap_half(close)
    up_close, up_away = pack(place, after(grad_out, close), frames, waits=True)
    share = after(share, up_close, valid, near)
    pieces = four_of_plane(share)
    away = after(away, pieces[1:], other_close)
    half_weights = [[weights, near, *pieces, *map(over_c, after(pieces, away))]]
    own = four_of(after(close, away), away)
    other_away = swap_half(away)
    others = [(other_close, 0), (over_c(other_close), 1)]
    params = jnp.stack([gains, shifts + biases, decays], axis=1)
    own_params = params.reshape(LAYERS * 3 * width // LANES, LANES)
    params = None

    def gather(array, axes):
        return lax.all_gather(array, axes, tiled=True)

    weight = half_weights[0]
    early = jnp.concatenate([own_blocks, other_blocks[:2]])
    z, own_flat = project(place, frames, own + others, early, weight, 0, flat=own)
    others += [(other_away, 0), (over_c(after(other_away, z)[frames:]), 0)]
    z, stats, other_flat = project(
        place,
        frames,
        others[2:],
        other_blocks[2:],
        weight,
        0,
        z,
        valid,
        params=own_params,
        flat=others,
    )
    z = [z]
    stats = gather(stats, ("h", "c"))
    share = over_c(lax.ppermute(after(far_share(1), stats), ("h", "c"), DIAGONAL))
    stats = gather(stats, ("y", "x"))
    x, states, slopes, params = recur(0, place, gate, z, stats, None, valid, own_flat, False)
    own_near, other_near = over_c(after(own_flat, z[0])), over_c(after(other_flat, z[0]))
    x_near = over_c(x)
    own_split = prepare(place, after(own_flat, x_near), own_near)
    other_split = prepare(place, after(other_flat, x_near), other_near)
    saved = [(own_split, other_split, z, stats, states, slopes)]

    pieces = four_of_plane(after(share, slopes, own_near, other_near))
    near = [weights, near]
    other = swap_half(x)
    x_own = after(x, own_split[0], other_split[0])
    z, *_ = project(place, frames, [(x_own, None)], own_blocks, near, 1)
    own_split = prepare(place, after(x, z), x_near)
    far = [*pieces, *map(over_c, after(pieces, own_split[0]))]
    up_away = over_h(after(up_away, own_split[0]))
    half_weights.append(near + far)
    z, stats = project(place, frames, [(other, None)], other_blocks, near, 1, z, valid)
    both = jnp.concatenate([own_blocks, other_blocks])
    z_far, stats = project(
        place,
        frames,
        [(x, None), (other, None)],
        both,
        far,
        1,
        None,
        valid,
        stats,
    )
    z = [z, z_far]
    stats = gather(gather(stats, ("y", "x")), ("h", "c"))
    upstream = four_of(up_close, after(up_away, stats))
    *output, states, slopes = recur(1, place, gate, z, stats, params, valid, x, True)
    other_near = over_c(after(other, slopes))
    saved.append((own_split, (other, other_near), z, stats, states, slopes))
    diagonal = over_c(over_h(output[3]))

    ups = upstream
    results = [None] * LAYERS
    for layer in range(LAYERS - 1, -1, -1):
        own_split, other_split, z, stats, states, slopes = saved[layer]
        weight = half_weights[layer]
        grad_pre, sums = back(layer, place, gate, z, stats, params, ups, states, slopes)
        sums = gather(sums, ("y", "x"))
        if layer == 0:
            come[0] = after(come[0], sums, away, output[1][0])
            later, go = step_of((in_hbm(stay[0]), come[0]), (in_hbm(stay[1]), come[1]))
            sums = after(sums, later)
            go = over_second(go)
        sums = gather(sums, ("h", "c"))
        grad_z, leaving, *terms, sums = norm_back(
            other_columns, place, grad_pre, z, params, valid, stats, sums, weight, layer,
            layer == 0,
        )
        leaving = over_c(leaving)
        if layer > 0:
            received = [swap_half(terms[0])]
            other_split = prepare(place, *after(other_split, grad_z))
            leaving = after(leaving, diagonal, other_split[0])
        else:
            received = [None, swap_half(terms[1])]
            later, go = step_of((later, after(go, grad_z)), hbm_outs=(0,))
            leaving = after(leaving, later)
            go = lax.ppermute(go, ("h", "c"), DIAGONAL)
            later = (later, go)
        *first, g_high, g_low = weight_rows(0, place, (grad_z, leaving), own_split, width)
        turned = (g_high, g_low)
        come = [plane_swap(first[1], 0)]
        if layer == 0:
            received[0] = swap_half(after(terms[0], received[1]))
        second = weight_rows(1, place, turned, other_split, width)
        come.append(plane_swap(second[1], 0))
        stay = (first[0], second[0])
        kept = own_terms(own_columns, place, after(grad_z, second[0]), ups, weight, layer)
        if layer > 0:
            away = over_h(after(output[2], kept))
            output = [(a, 0) for a in (output[0], over_c(output[1]), away, diagonal)]
        ups = [(kept, None)] + [(r, None) for r in received]
        results[layer] = lax.dynamic_index_in_dim(
            sums.reshape(3, 4, width), clip, axis=1, keepdims=False
        )

    sums = jnp.stack(results)
    sums = [sums[:, 0], sums[:, 1], sums[:, 2]]
    aways = merge(kept, 1, received[1], apart=True)
    later = (in_hbm(later[0]), over_c(after(later[1], aways[0])))
    come[0] = after(come[0], sums, later[1])
    far_near = over_c(lax.ppermute(aways[0], ("h", "c"), DIAGONAL))
    near_sum, far_sum, near_go, far_go = step_of(
        (in_hbm(stay[0]), come[0]), (in_hbm(stay[1]), come[1]), cut=2
    )
    near_go, far_go = over_second(near_go), over_second(far_go)
    (go,) = step_of((far_sum, after(far_go, far_near)), cut=0)
    (later,) = step_of(later, cut=0)
    later = after(later, go)
    go = over_h(go)
    later = plane_gather(later)
    (total,) = step_of((near_sum, near_go), cut=0)
    output = unpack(place, [(after(array, total), i) for array, i in output], frames, waited=True)
    close = merge(kept, 0, after(received[0], output))
    far = over_c(over_h(after(aways[1], go)))
    (share,) = step_of((total, after(go, close, *later[1:])), cut=0)
    grad_weights = assemble(place, after(later, share), 1)
    gathered = plane_gather(share, grad_weights)
    grad_in = [(close, 0), (over_c(close[frames:]), 0), (far_near, 0), (far, 0)]
    grad_in = unpack(place, grad_in, frames)
    grad_weights = assemble(place, after(gathered, grad_in), 0, grad_weights)
    return (output, grad_in, grad_weights, *sums, sums[1])


def gelu_slope(value):
    return (
        0.5 * (1.0 + jax.scipy.special.erf(value / ROOT_TWO))
        + value * jnp.exp(-0.5 * value * value) / ROOT_TWO_PI
    )


def recur_step(decay, state, inputs):
    drive_t, valid_t = inputs
    pre = drive_t + decay * state
    state = state + valid_t * (jax.nn.gelu(pre, approximate=False) - state)
    return (state, state)


def back_step(decay, carry, inputs):
    upstream_t, valid_t, pre_t = inputs
    total = upstream_t + carry
    grad_pre = total * valid_t * gelu_slope(pre_t)
    carry = total * (1.0 - valid_t) + grad_pre * decay
    return (carry, grad_pre)


def add_piece(weight, piece):
    return jnp.dot(weight, piece, precision=HIGH, preferred_element_type=jnp.float32)


def weight_columns(grad_pre_norm, piece):
    return jnp.einsum("jf,kf->jk", grad_pre_norm, piece, precision=HIGH)


def split_features(inputs, weights, gains, shifts, decays, biases, lengths, frame_mask, grad_out):
    width, slots = inputs.shape
    clips, frames_len = frame_mask.shape
    frames = jnp.arange(frames_len, dtype=jnp.int32)
    valid_grid = (
        (frames[None, :] < lengths[:, None]) & ((frame_mask == 1) | (frames[None, :] == 0))
    ).astype(jnp.float32)
    valid = valid_grid.reshape(-1)
    valid_row = valid[None, :]
    valid_time = jnp.broadcast_to(valid_grid.T[:, :, None], (frames_len, clips, width)).reshape(
        frames_len, clips * width
    )
    count_local = jnp.sum(valid)

    def to_time(array):
        return jnp.transpose(array.reshape(width, clips, frames_len), (2, 1, 0)).reshape(
            frames_len, clips * width
        )

    def from_time(array):
        return jnp.transpose(array.reshape(frames_len, clips, width), (2, 1, 0)).reshape(
            width, slots
        )

    layer_in = inputs
    saved = []
    for layer_no in range(LAYERS):
        weight = weights[layer_no]
        gathered = lax.all_gather(layer_in, "neuron", axis=0, tiled=True)
        pre_norm = add_piece(weight, gathered)
        first_sum, count = lax.psum((jnp.sum(valid_row * pre_norm, axis=1), count_local), "batch")
        mean = first_sum / count
        centered = pre_norm - mean[:, None]
        var = lax.psum(jnp.sum(valid_row * centered * centered, axis=1), "batch") / count
        inv_std = lax.rsqrt(var + EPS)
        zhat = (pre_norm - mean[:, None]) * inv_std[:, None]
        drive = gains[layer_no][:, None] * zhat + (shifts[layer_no] + biases[layer_no])[:, None]
        drive_time = to_time(drive)
        decay_wide = jnp.tile(decays[layer_no], clips)
        start_state = jnp.zeros((clips * width,), jnp.float32)
        _, states = lax.scan(
            partial(recur_step, decay_wide), start_state, (drive_time, valid_time), unroll=8
        )
        saved.append((gathered, zhat, inv_std, drive_time, states, count))
        layer_in = layer_in + valid_row * from_time(states)
    upstream = grad_out
    grad_parts = [None] * LAYERS
    for layer_no in range(LAYERS - 1, -1, -1):
        gathered, zhat, inv_std, drive_time, states, count = saved[layer_no]
        decay_wide = jnp.tile(decays[layer_no], clips)
        gain = gains[layer_no]
        previous = jnp.concatenate([jnp.zeros_like(states[:1]), states[:-1]], axis=0)
        pre_time = drive_time + decay_wide[None, :] * previous
        grad_state = to_time(valid_row * upstream)
        start_carry = jnp.zeros((clips * width,), jnp.float32)
        _, grad_pre_time = lax.scan(
            partial(back_step, decay_wide),
            start_carry,
            (grad_state, valid_time, pre_time),
            reverse=True,
            unroll=8,
        )
        decay_local = jnp.sum(
            jnp.sum(grad_pre_time * previous, axis=0).reshape(clips, width), axis=0
        )
        grad_pre = from_time(grad_pre_time)
        gain_local = jnp.sum(grad_pre * zhat, axis=1)
        shift_local = jnp.sum(grad_pre, axis=1)
        grad_gain, grad_shift, grad_decay = lax.psum(
            (gain_local, shift_local, decay_local), "batch"
        )
        grad_pre_norm = (gain * inv_std)[:, None] * (
            grad_pre - valid_row * (grad_shift[:, None] + zhat * grad_gain[:, None]) / count
        )
        weight_local = weight_columns(grad_pre_norm, gathered)
        input_terms = jnp.einsum("jk,jf->kf", weights[layer_no], grad_pre_norm, precision=HIGH)
        input_grad = lax.psum_scatter(input_terms, "neuron", scatter_dimension=0, tiled=True)
        grad_weight = lax.psum(weight_local, "batch")
        upstream = upstream + input_grad
        grad_parts[layer_no] = (grad_weight, grad_gain, grad_shift, grad_decay)
    grad_weights = jnp.stack([grad_parts[layer_no][0] for layer_no in range(LAYERS)])
    grad_gains = jnp.stack([grad_parts[layer_no][1] for layer_no in range(LAYERS)])
    grad_shifts = jnp.stack([grad_parts[layer_no][2] for layer_no in range(LAYERS)])
    grad_decays = jnp.stack([grad_parts[layer_no][3] for layer_no in range(LAYERS)])
    return (layer_in, upstream, grad_weights, grad_gains, grad_shifts, grad_decays, grad_shifts)


def solution(mesh):
    if (mesh.shape["batch"], mesh.shape["neuron"]) == (4, 8):
        cut = Mesh(mesh.devices.reshape(2, 2, 2, 2, 2), ("y", "x", "h", "l", "c"))
        batch, neuron, body = ("y", "x"), ("h", "l", "c"), half_features
    else:
        cut, batch, neuron, body = mesh, "batch", "neuron", split_features
    in_specs = (
        P(neuron, batch),
        P(None, neuron, None),
        P(None, neuron),
        P(None, neuron),
        P(None, neuron),
        P(None, neuron),
        P(batch),
        P(batch, None),
        P(neuron, batch),
    )
    out_specs = (
        P(neuron, batch),
        P(neuron, batch),
        P(None, neuron, None),
        P(None, neuron),
        P(None, neuron),
        P(None, neuron),
        P(None, neuron),
    )
    return jax.shard_map(
        body, mesh=cut, in_specs=in_specs, out_specs=out_specs, check_vma=False
    )
```

```python
from functools import partial
import math

import jax
import jax.numpy as jnp
from jax import lax
from jax.experimental import pallas as pl
from jax.experimental.pallas import tpu as pltpu
from jax.sharding import Mesh, PartitionSpec as P

LAYERS = 2
EPS = 1e-05
HIGH = lax.Precision.HIGHEST
ROOT_TWO = math.sqrt(2.0)
ROOT_TWO_PI = math.sqrt(2.0 * math.pi)
F32 = jnp.float32
BF16 = jnp.bfloat16
LANES = 128
VMEM_LIMIT = 24 * 1024 * 1024
SMEM_SPEC = pl.BlockSpec(memory_space=pltpu.SMEM)
VMEM_SPEC = pl.BlockSpec(memory_space=pltpu.VMEM)


FLIP2 = [(0, 1), (1, 0)]
DIAGONAL = [(0, 3), (1, 2), (2, 1), (3, 0)]


def swap_half(array):
    return lax.ppermute(array, "l", FLIP2)


def after(value, *others):
    return lax.optimization_barrier((value, others))[0]


def split(value):
    high = value.astype(BF16)
    return high, (value - high.astype(F32)).astype(BF16)


def dot(a, b, dims):
    return lax.dot_general(a, b, (dims, ((), ())), preferred_element_type=F32)


NT = ((1,), (1,))
NN = ((1,), (0,))


def in_hbm(array):
    return pltpu.with_memory_space_constraint(array, pltpu.HBM)


def call(body, out_shape, hbm_outs=(), **kwargs):
    if hbm_outs:
        out_shape = [
            pltpu.HBM(a.shape, a.dtype) if i in hbm_outs else a for i, a in enumerate(out_shape)
        ]
    return pl.pallas_call(
        body,
        out_shape=out_shape,
        compiler_params=pltpu.CompilerParams(vmem_limit_bytes=VMEM_LIMIT),
        **kwargs,
    )


def cost(flops, byte_count):
    return pl.CostEstimate(flops=int(flops) // 64, bytes_accessed=int(byte_count) // 64, transcendentals=0)


def pack_body(frames, place_ref, in_ref, near_ref, far_ref, turned):
    slots = in_ref.shape[1]
    for start in range(0, slots, LANES):
        turned[start : start + LANES, :] = in_ref[:, start : start + LANES].T
    for rel in range(4):
        first = pl.multiple_of(place_ref[rel] * frames, 8)
        out = (near_ref, far_ref)[rel // 2]
        out[(rel % 2) * frames : (rel % 2 + 1) * frames, :] = turned[pl.ds(first, frames), :]


def pack(place, array, frames, waits=False):
    width, slots = array.shape
    out = jax.ShapeDtypeStruct((2 * frames, width), F32)
    return call(
        partial(pack_body, frames),
        grid=(1,),
        out_shape=[out, out],
        in_specs=[SMEM_SPEC, pl.BlockSpec((width, slots), lambda i: (0, 0))],
        out_specs=[pl.BlockSpec(out.shape, lambda i: (0, 0))] * 2,
        scratch_shapes=[pltpu.VMEM((slots, width), F32)],
        hbm_outs=(0, 1) if waits else (),
        cost_estimate=cost(0, 8 * width * slots),
        name="pack",
    )(place, in_hbm(array))


def part_spec(part, frames):
    array, i = part
    if i is None:
        return pl.BlockSpec(array.shape, lambda *_: (0,) * array.ndim)
    return pl.BlockSpec((frames, array.shape[1]), lambda *_: (i, 0))


def arrays_of(parts):
    return [array for array, _ in parts]


def unpack_body(frames, place_ref, *refs):
    ins, out_ref, turned = refs[:4], refs[4], refs[5]
    slots = out_ref.shape[1]
    for rel in range(4):
        first = pl.multiple_of(place_ref[rel] * frames, 8)
        turned[pl.ds(first, frames), :] = ins[rel][...]
    for start in range(0, slots, LANES):
        out_ref[:, start : start + LANES] = turned[start : start + LANES, :].T


def unpack(place, parts, frames, waited=False):
    width = parts[0][0].shape[1]
    slots = 4 * frames
    return call(
        partial(unpack_body, frames),
        grid=(1,),
        out_shape=jax.ShapeDtypeStruct((width, slots), F32),
        in_specs=[SMEM_SPEC] + [part_spec(part, frames) for part in parts],
        out_specs=pl.BlockSpec((width, slots), lambda i: (0, 0)),
        scratch_shapes=[pltpu.VMEM((slots, width), F32)],
        cost_estimate=cost(0, 8 * width * slots),
        name="unpack",
    )(place, *[in_hbm(a) if waited else a for a in arrays_of(parts)])


def merge_body(kept_ref, come_ref, *outs):
    frames, columns = kept_ref.shape
    width = columns // 2
    for i in range(2):
        some = slice(i * width, (i + 1) * width)
        if len(outs) > 1:
            outs[i][...] = kept_ref[:, some] + come_ref[:, some]
            continue
        (out_ref,) = outs
        out_ref[i * frames : (i + 1) * frames, :] = kept_ref[:, some] + come_ref[:, some]


def merge(kept, half, come, apart=False):
    frames, columns = come.shape
    rows, n = (frames, 2) if apart else (2 * frames, 1)
    outs = call(
        merge_body,
        hbm_outs=(0, 1) if apart else (),
        grid=(1,),
        out_shape=[jax.ShapeDtypeStruct((rows, columns // 2), F32)] * n,
        in_specs=[
            pl.BlockSpec((frames, columns), lambda i: (0, half)),
            pl.BlockSpec((frames, columns), lambda i: (0, 0)),
        ],
        out_specs=[pl.BlockSpec((rows, columns // 2), lambda i: (0, 0))] * n,
        cost_estimate=cost(0, 12 * frames * columns),
        name="merge",
    )(kept, come)
    return outs if apart else outs[0]


def project_body(n_parts, n_flat, spots, n_weights, first, with_acc, with_stats, with_params, cols_ref, place_ref, *refs):
    del cols_ref

    def take(n):
        nonlocal refs
        some, refs = refs[:n], refs[n:]
        return some

    parts, flat_parts, weights = take(n_parts), take(n_flat), take(n_weights)
    acc, valid, stats_in, params = take(with_acc), take(with_stats > 0), take(with_stats > 1), take(with_params)
    (out_ref,) = take(1)
    stats, flat = take(with_stats > 0), take(n_flat > 0)
    x_high, x_low, far_ref = refs
    step = pl.program_id(0)
    width = x_high.shape[2]

    @pl.when(step == 0)
    def _():
        for block, part in zip(spots, parts):
            for start in range(0, part.shape[1], width):
                high, low = split(part[:, start : start + width])
                x_high[block + start // width] = high
                x_low[block + start // width] = low
        column = 0
        for part in flat_parts:
            flat[0][:, column : column + part.shape[1]] = part[...]
            column += part.shape[1]
        if with_acc:
            out_ref[...] = acc[0][...]
        else:
            out_ref[...] = jnp.zeros_like(out_ref)

    stacked = jnp.concatenate([x_high[step], x_low[step], x_high[step]], axis=1)
    for block, weight in enumerate(weight_blocks(place_ref, weights, far_ref)):
        w_high, w_low = split(weight)
        columns = slice(block * width, (block + 1) * width)
        out_ref[:, columns] += dot(stacked, jnp.concatenate([w_high, w_high, w_low], axis=1), NT)

    if with_stats:
        (stats_ref,) = stats

        @pl.when(step == pl.num_programs(0) - 1)
        def _():
            if stats_in:
                stats_ref[...] = stats_in[0][...]
            own = jnp.sum(valid[0][...], axis=0, keepdims=True)
            per = width // LANES
            for row in range(out_ref.shape[1] // LANES):
                z = out_ref[:, row * LANES : (row + 1) * LANES]
                total = jnp.sum(valid[0][...] * z, axis=0, keepdims=True)
                centred = valid[0][...] * (z - total / own)
                squares = jnp.sum(centred * centred, axis=0, keepdims=True)
                at = place_ref[first + row // per] * per + row % per
                stats_ref[0, pl.ds(at, 1), :] = total
                stats_ref[1, pl.ds(at, 1), :] = squares
                stats_ref[2, pl.ds(at, 1), :] = own
            if with_params:
                rest = params[0].shape[0] - 8
                stats_ref[3] = params[0][:8, :]
                stats_ref[4] = jnp.zeros_like(stats_ref[4])
                stats_ref[4, :rest, :] = params[0][8:, :]


def weight_specs(weights, layer, pairs=2):
    specs = []
    for weight in weights:
        if weight.ndim == 3:
            shape = (1, weight.shape[1], pairs * weight.shape[1])
            specs.append(pl.BlockSpec(shape, lambda s, cols, *_: (layer, 0, cols[s])))
        else:
            shape = (weight.shape[0], pairs * 4 * weight.shape[0])
            specs.append(pl.BlockSpec(shape, lambda s, cols, *_: (0, cols[s])))
    return specs


def far_scratch(width, pairs=2):
    return pltpu.VMEM((2, width, pairs * width), F32)


def weight_blocks(place_ref, refs, far_ref):
    near = [ref[0] for ref in refs if len(ref.shape) == 3]
    pieces = [ref for ref in refs if len(ref.shape) == 2]
    far = []
    for i in range(len(pieces) // 4):
        for rel, piece in enumerate(pieces[4 * i : 4 * i + 4]):
            rows = piece.shape[0]
            row = 2 * (place_ref[4] ^ (rel // 2)) + (place_ref[5] ^ (rel % 2))
            far_ref[i, pl.ds(pl.multiple_of(row * rows, rows), rows), :] = piece[...]
        far.append(far_ref[i])
    return near + far


def project(
    place, frames, parts, blocks, weights, layer, acc=None, valid=None, stats=None, params=None, flat=()
):
    near = weights[0].ndim == 3
    units = sum(1 if w.ndim == 3 else 0.25 for w in weights)
    width = weights[0].shape[1] if near else 4 * weights[0].shape[0]
    n = blocks.shape[0]
    spots, block = [], 0
    for array, _ in parts:
        spots.append(block)
        block += array.shape[1] // width
    full = pl.BlockSpec(memory_space=pltpu.VMEM)
    in_specs = [part_spec(part, frames) for part in (*parts, *flat)]
    in_specs += weight_specs(weights, layer, 1)
    operands = arrays_of(parts) + arrays_of(flat) + [in_hbm(w) for w in weights]
    array = jax.ShapeDtypeStruct((frames, int(units) * width), F32)
    array_spec = pl.BlockSpec(array.shape, lambda s, cols, place: (0, 0))
    out_shape, out_specs = [array], [array_spec]
    if acc is not None:
        in_specs.append(array_spec)
        operands.append(in_hbm(acc))
    if valid is not None:
        in_specs.append(full)
        operands.append(valid)
        shape = (3 if params is None else 5, 4 * width // LANES, LANES)
        out_shape.append(jax.ShapeDtypeStruct(shape, F32))
        out_specs.append(pl.BlockSpec(shape, lambda s, cols, place: (0, 0, 0)))
    for extra in (stats, params):
        if extra is not None:
            in_specs.append(full)
            operands.append(extra)
    if flat:
        out_shape.append(jax.ShapeDtypeStruct((frames, 4 * width), F32))
        out_specs.append(pl.BlockSpec((frames, 4 * width), lambda s, cols, place: (0, 0)))
    return call(
        partial(
            project_body,
            len(parts),
            len(flat),
            spots,
            len(weights),
            0 if near else 2,
            acc is not None,
            (valid is not None) + (stats is not None),
            params is not None,
        ),
        grid_spec=pltpu.PrefetchScalarGridSpec(
            num_scalar_prefetch=2,
            grid=(n,),
            in_specs=in_specs,
            out_specs=out_specs,
            scratch_shapes=[pltpu.VMEM((n, frames, width), BF16)] * 2 + [far_scratch(width, 1)],
        ),
        out_shape=out_shape,
        hbm_outs=(0, len(out_shape) - 1) if flat else (0,),
        cost_estimate=cost(6 * frames * n * width * units * width, 4 * n * width * units * width),
        name="project",
    )(blocks, place, *operands)


def to_relative(place_ref, spread, rows_ref, value, slot):
    per = value.shape[0] // 4
    spread[...] = value
    for rel in range(4):
        first = place_ref[rel] * per
        for row in range(per):
            rows_ref[slot, rel * per + row : rel * per + row + 1, :] = spread[
                pl.ds(first + row, 1), :
            ]


def tree(values):
    while len(values) > 1:
        values = [a + b for a, b in zip(values[::2], values[1::2])]
    return values[0]


def gathered(ref, slot):
    return [ref[i] for i in range(slot, ref.shape[0], ref.shape[0] // 16)]


def norm_terms(stats_ref):
    each = [gathered(stats_ref, slot) for slot in range(3)]
    totals, squares, owns = each
    count = tree(owns)
    mean = tree(totals) / count
    away = [total / own - mean for total, own in zip(totals, owns)]
    spread = tree([s + n * a * a for s, n, a in zip(squares, owns, away)])
    return count, mean, lax.rsqrt(spread / count + EPS)


CHUNKS = 4


def columns_of(refs, row):
    for ref in refs:
        if row * LANES < ref.shape[1]:
            return ref[:, row * LANES : (row + 1) * LANES]
        row -= ref.shape[1] // LANES


def recur_body(n_z, last, layer, spread_params, place_ref, gate_ref, *refs):
    z_refs, refs = refs[:n_z], refs[n_z:]
    (stats_ref, params_ref, valid_ref, x_ref), refs = refs[:4], refs[4:]
    outs, refs = refs[: 1 + 3 * last], refs[1 + 3 * last :]
    if spread_params:
        state_ref, slope_ref, params_out, rows, spread, held, drive_s, state_s, slope_s = refs
    else:
        state_ref, slope_ref, rows, spread, held, drive_s, state_s, slope_s = refs
    frames, features = x_ref.shape
    blocks = features // LANES
    per = blocks // 4
    chunk = pl.program_id(0)

    @pl.when(chunk == 0)
    def _():
        if spread_params:
            for rel in range(4):
                first = place_ref[rel] * (stats_ref.shape[0] // 16) + 3
                for row in range(LAYERS * 3 * per):
                    at = rel * per + row % per
                    params_out[row // per, at : at + 1, :] = stats_ref[
                        first + row // 8, row % 8 : row % 8 + 1, :
                    ]
            params = [params_out[3 * layer + i] for i in range(3)]
        else:
            params = [params_ref[3 * layer + i] for i in range(3)]
        _, mean, inv_std = norm_terms(stats_ref)
        to_relative(place_ref, spread, rows, mean, 0)
        to_relative(place_ref, spread, rows, inv_std, 1)
        rows[1] = rows[1] * params[0]
        rows[2] = params[1]
        rows[3] = params[2]
        held[...] = jnp.zeros_like(held)

    for row in range(blocks):
        drive_s[row * frames : (row + 1) * frames, :] = (
            columns_of(z_refs, row) - rows[0, row : row + 1, :]
        ) * rows[1, row : row + 1, :] + rows[2, row : row + 1, :]
    decay = rows[3]

    def step(t, state):
        at = pl.ds(t, blocks, stride=frames)
        pre = drive_s[at, :] + decay * state
        half = 0.5 + 0.5 * lax.erf(pre * (1.0 / ROOT_TWO))
        gate = gate_ref[chunk * frames + t] > 0.0
        slope = half + pre * jnp.exp(-0.5 * pre * pre) * (1.0 / ROOT_TWO_PI)
        state = jnp.where(gate, pre * half, state)
        state_s[at, :] = state
        slope_s[at, :] = jnp.where(gate, slope, 0.0)
        return state

    held[...] = lax.fori_loop(0, frames, step, held[...], unroll=8)
    valid = valid_ref[...]
    for row in range(blocks):
        lanes = slice(row * LANES, (row + 1) * LANES)
        state = state_s[row * frames : (row + 1) * frames, :]
        state_ref[:, lanes] = state
        slope_ref[:, lanes] = slope_s[row * frames : (row + 1) * frames, :]
        value = x_ref[:, lanes] + valid * state
        out, at = (outs[row // per], row % per) if last else (outs[0], row)
        out[:, at * LANES : (at + 1) * LANES] = value


def recur(layer, place, gate, z, stats, params, valid, x, last):
    frames, features = x.shape
    blocks = features // LANES
    some = frames // CHUNKS
    whole = lambda array: pl.BlockSpec(array.shape, lambda i: (0,) * array.ndim)
    by_chunk = lambda array: pl.BlockSpec((some, array.shape[1]), lambda i: (i, 0))
    full = jax.ShapeDtypeStruct((frames, features), F32)
    piece = jax.ShapeDtypeStruct((frames, features // 4), F32)
    out_shape = [piece] * 4 if last else [full]
    out_shape += [full, full]
    out_specs = [by_chunk(a) for a in out_shape]
    spread_params = params is None
    if spread_params:
        out_shape.append(jax.ShapeDtypeStruct((3 * LAYERS, blocks, LANES), F32))
        out_specs.append(whole(out_shape[-1]))
        params = valid
    return call(
        partial(recur_body, len(z), last, layer, spread_params),
        grid=(CHUNKS,),
        in_specs=[SMEM_SPEC, SMEM_SPEC]
        + [by_chunk(a) for a in z]
        + [whole(a) for a in (stats, params)]
        + [by_chunk(a) for a in (valid, x)],
        out_specs=out_specs,
        out_shape=out_shape,
        hbm_outs=tuple(range(len(out_shape) - spread_params)) if last else (1, 2),
        scratch_shapes=[
            pltpu.VMEM((4, blocks, LANES), F32),
            pltpu.VMEM((blocks, LANES), F32),
            pltpu.VMEM((blocks, LANES), F32),
        ]
        + [pltpu.VMEM((blocks * some, LANES), F32)] * 3,
        cost_estimate=cost(100 * frames * features, 20 * frames * features),
        name="recur",
    )(place, gate, *[in_hbm(a) for a in z], stats, params, valid, in_hbm(x))


def back_body(n_z, n_ups, spots, layer, place_ref, gate_ref, *refs):
    z_refs, refs = refs[:n_z], refs[n_z:]
    (stats_ref, params_ref), refs = refs[:2], refs[2:]
    ups, (state_ref, slope_ref), refs = refs[:n_ups], refs[n_ups : n_ups + 2], refs[n_ups + 2 :]
    grad_ref, sums_ref, rows, spread, held, up_s, state_s, slope_s = refs
    frames, features = state_ref.shape
    blocks = features // LANES
    per = blocks // 4
    tall = frames + 8
    step_no = pl.program_id(0)
    chunk = pl.num_programs(0) - 1 - step_no

    @pl.when(step_no == 0)
    def _():
        _, mean, inv_std = norm_terms(stats_ref)
        to_relative(place_ref, spread, rows, mean, 0)
        to_relative(place_ref, spread, rows, inv_std, 1)
        held[...] = jnp.zeros_like(held)

    for row in range(blocks):
        lanes = slice(row * LANES, (row + 1) * LANES)
        base = row * frames
        up = None
        for (_, column), part in zip(spots, ups):
            if column <= row * LANES < column + part.shape[1]:
                value = part[:, row * LANES - column : (row + 1) * LANES - column]
                up = value if up is None else up + value
        up_s[base : base + frames, :] = up
        state_s[row * tall : row * tall + 8, :] = jnp.zeros((8, LANES), F32)
        state_s[row * tall + 8 : (row + 1) * tall, :] = state_ref[:, lanes]
        slope_s[base : base + frames, :] = slope_ref[:, lanes]
    decay = params_ref[3 * layer + 2]

    def step(i, carry):
        t = frames - 1 - i
        at = pl.ds(t, blocks, stride=frames)
        slope = slope_s[at, :]
        gate = gate_ref[chunk * frames + t]
        total = gate * up_s[at, :] + carry
        up_s[at, :] = total * slope
        return total * (slope * decay + (1.0 - gate))

    held[0] = lax.fori_loop(0, frames, step, held[0], unroll=8)
    held[4] += held[1] * state_s[pl.ds(tall - 1, blocks, stride=tall), :]
    held[1] = up_s[pl.ds(0, blocks, stride=frames), :]
    for row in range(blocks):
        lanes = slice(row * LANES, (row + 1) * LANES)
        grad = up_s[row * frames : (row + 1) * frames, :]
        grad_ref[:, lanes] = grad
        zhat = (columns_of(z_refs, row) - rows[0, row : row + 1, :]) * rows[1, row : row + 1, :]
        before = state_s[row * tall + 7 : row * tall + 7 + frames, :]
        for slot, value in enumerate((grad * zhat, grad, grad * before)):
            held[2 + slot, row : row + 1, :] += jnp.sum(value, axis=0, keepdims=True)

    @pl.when(chunk == 0)
    def _():
        for row in range(blocks):
            at = place_ref[row // per] * per + row % per
            for slot in range(3):
                sums_ref[slot, pl.ds(at, 1), :] = held[2 + slot, row : row + 1, :]


def spots_of_sum(parts, width):
    spots, column = [], 0
    for array, _ in parts:
        spots.append((0, column % (4 * width)))
        column += array.shape[1]
    return spots


def back(layer, place, gate, z, stats, params, ups, states, slopes):
    frames, features = states.shape
    width = features // 4
    blocks = features // LANES
    some = frames // CHUNKS
    whole = lambda array: pl.BlockSpec(array.shape, lambda i: (0,) * array.ndim)

    def by_chunk(array, first=0):
        return pl.BlockSpec(
            (some, array.shape[1]), lambda i: ((first or 0) * CHUNKS + CHUNKS - 1 - i, 0)
        )

    out_shape = [
        jax.ShapeDtypeStruct((frames, features), F32),
        jax.ShapeDtypeStruct((3, blocks, LANES), F32),
    ]
    return call(
        partial(back_body, len(z), len(ups), spots_of_sum(ups, width), layer),
        grid=(CHUNKS,),
        in_specs=[SMEM_SPEC] * 2
        + [by_chunk(a) for a in z]
        + [whole(a) for a in (stats, params)]
        + [by_chunk(*up) for up in ups]
        + [by_chunk(a) for a in (states, slopes)],
        out_specs=[by_chunk(out_shape[0]), whole(out_shape[1])],
        out_shape=out_shape,
        scratch_shapes=[
            pltpu.VMEM((2, blocks, LANES), F32),
            pltpu.VMEM((blocks, LANES), F32),
            pltpu.VMEM((5, blocks, LANES), F32),
            pltpu.VMEM((blocks * some, LANES), F32),
            pltpu.VMEM((blocks * (some + 8), LANES), F32),
            pltpu.VMEM((blocks * some, LANES), F32),
        ],
        cost_estimate=cost(30 * frames * features, 20 * frames * features),
        name="back",
    )(
        place,
        gate,
        *[in_hbm(a) for a in z],
        stats,
        params,
        *arrays_of(ups),
        in_hbm(states),
        in_hbm(slopes),
    )


def input_terms(high_s, low_s, weights):
    left, right = [], []
    for block, weight in enumerate(weights):
        w_high, w_low = split(weight)
        left += [high_s[block], low_s[block], high_s[block]]
        right += [w_high, w_high, w_low]
    return dot(jnp.concatenate(left, axis=1), jnp.concatenate(right, axis=0), NN)


def norm_back_body(n_z, split_terms, layer, cols_ref, place_ref, grad_ref, *refs):
    del cols_ref
    z_refs, refs = refs[:n_z], refs[n_z:]
    params_ref, valid_ref, stats_ref, sums_ref, *refs = refs
    weights, refs = refs[:10], refs[10:]
    if split_terms:
        out_ref, leave_ref, near_term_ref, far_term_ref, sums_out_ref, *refs = refs
        term_refs, starts = (far_term_ref, near_term_ref), (0, 0)
    else:
        out_ref, leave_ref, term_ref, sums_out_ref, *refs = refs
        term_refs, starts = (term_ref, term_ref), (2 * grad_ref.shape[1] // 4, 0)
    rows, spread, high_s, low_s, far_ref = refs
    blocks = grad_ref.shape[1] // LANES
    width = high_s.shape[2]
    per = width // LANES

    @pl.when(pl.program_id(0) == 0)
    def _():
        count, mean, inv_std = norm_terms(stats_ref)
        to_relative(place_ref, spread, rows, mean, 0)
        to_relative(place_ref, spread, rows, inv_std, 1)
        rows[2] = rows[1] * params_ref[3 * layer]
        sums = [tree(gathered(sums_ref, slot)) for slot in range(3)]
        for slot in range(3):
            sums_out_ref[slot] = sums[slot]
        to_relative(place_ref, spread, rows, sums[0] / count, 3)
        to_relative(place_ref, spread, rows, sums[1] / count, 4)
        valid = valid_ref[...]
        for row in range(blocks):
            lanes = slice(row * LANES, (row + 1) * LANES)
            one = lambda slot: rows[slot, row : row + 1, :]
            zhat = (columns_of(z_refs, row) - one(0)) * one(1)
            value = one(2) * (grad_ref[:, lanes] - valid * (one(4) + zhat * one(3)))
            out_ref[:, lanes] = value
            if (row // per) % 2:
                at = (row // per // 2) * width + (row % per) * LANES
                leave_ref[:, at : at + LANES] = value
            high, low = split(value)
            inner = slice((row % per) * LANES, (row % per + 1) * LANES)
            high_s[row // per, :, inner] = high
            low_s[row // per, :, inner] = low

    value = input_terms(high_s, low_s, weight_blocks(place_ref, weights, far_ref))
    for step, (term_ref, first) in enumerate(zip(term_refs, starts)):

        @pl.when(pl.program_id(0) == step)
        def _():
            for pair in range(2):
                at = pl.multiple_of(((place_ref[0] & 1) ^ pair) * width, width)
                term_ref[:, pl.ds(first + at, width)] = value[
                    :, pair * width : (pair + 1) * width
                ]


def norm_back(columns, place, grad, z, params, valid, stats, sums, weights, layer, split_terms):
    frames, features = grad.shape
    width = features // 4
    blocks = features // LANES
    whole = lambda array: pl.BlockSpec(array.shape, lambda s, cols, place: (0,) * array.ndim)
    operands = [grad, *[in_hbm(a) for a in z], params, valid, stats, sums]
    full = jax.ShapeDtypeStruct((frames, features), F32)
    half = jax.ShapeDtypeStruct((frames, 2 * width), F32)
    terms = [half, half] if split_terms else [full]
    out_shape = [full, half, *terms, jax.ShapeDtypeStruct((3, blocks, LANES), F32)]
    return call(
        partial(norm_back_body, len(z), split_terms, layer),
        grid_spec=pltpu.PrefetchScalarGridSpec(
            num_scalar_prefetch=2,
            grid=(2,),
            in_specs=[whole(a) for a in operands] + weight_specs(weights, layer),
            out_specs=[whole(a) for a in out_shape],
            scratch_shapes=[
                pltpu.VMEM((5, blocks, LANES), F32),
                pltpu.VMEM((blocks, LANES), F32),
                pltpu.VMEM((4, frames, width), BF16),
                pltpu.VMEM((4, frames, width), BF16),
                far_scratch(width),
            ],
        ),
        out_shape=out_shape,
        hbm_outs=(0, 2) if split_terms else (0,),
        cost_estimate=cost(6 * frames * features * features, 4 * features * features),
        name="norm_back",
    )(columns, place, *operands, *[in_hbm(w) for w in weights])


def own_terms_body(n_ups, spots, cols_ref, place_ref, grad_ref, *refs):
    del cols_ref
    ups, refs = refs[:n_ups], refs[n_ups:]
    weights, refs = refs[:10], refs[10:]
    out_ref, high_s, low_s, far_ref = refs
    width = high_s.shape[2]
    step = pl.program_id(0)

    @pl.when(step == 0)
    def _():
        for block in range(4):
            high, low = split(grad_ref[:, block * width : (block + 1) * width])
            high_s[block] = high
            low_s[block] = low

    value = input_terms(high_s, low_s, weight_blocks(place_ref, weights, far_ref))
    for pair in range(2):
        at = pl.multiple_of(((place_ref[0] & 1) ^ pair) * width, width)
        out_ref[:, pl.ds(at, width)] = value[:, pair * width : (pair + 1) * width]
    for half in range(2):

        @pl.when(step == half)
        def _():
            first = 2 * half * width
            for (_, column), up in zip(spots, ups):
                low = max(column, first)
                high = min(column + up.shape[1], first + 2 * width)
                if low < high:
                    out_ref[:, low - first : high - first] += up[:, low - column : high - column]


def own_terms(columns, place, grad, ups, weights, layer):
    frames, features = grad.shape
    width = features // 4
    whole = lambda array: pl.BlockSpec(array.shape, lambda s, cols, place: (0,) * array.ndim)
    step_block = pl.BlockSpec((frames, 2 * width), lambda s, cols, place: (0, s))
    return call(
        partial(own_terms_body, len(ups), spots_of_sum(ups, width)),
        grid_spec=pltpu.PrefetchScalarGridSpec(
            num_scalar_prefetch=2,
            grid=(2,),
            in_specs=[whole(grad)]
            + [part_spec(up, frames) for up in ups]
            + weight_specs(weights, layer),
            out_specs=step_block,
            scratch_shapes=[pltpu.VMEM((4, frames, width), BF16)] * 2 + [far_scratch(width)],
        ),
        out_shape=jax.ShapeDtypeStruct((frames, features), F32),
        cost_estimate=cost(6 * frames * features * features, 4 * features * features),
        name="own_terms",
    )(columns, place, in_hbm(grad), *arrays_of(ups), *[in_hbm(w) for w in weights])


def prepare_body(lists_ref, place_ref, own_ref, near_ref, high_ref, low_ref):
    del lists_ref
    padded = high_ref.shape[0] // 2
    width = high_ref.shape[1] // 2
    for clip, part in enumerate((own_ref, near_ref)):
        rows = part.shape[0]
        for dc in range(2):
            at = pl.multiple_of((place_ref[6] ^ clip ^ dc) * width, width)
            high, low = split(part[:, dc * width : (dc + 1) * width])
            high_ref[clip * padded : clip * padded + rows, pl.ds(at, width)] = high
            low_ref[clip * padded : clip * padded + rows, pl.ds(at, width)] = low
        zeros = jnp.zeros((padded - rows, 2 * width), BF16)
        high_ref[clip * padded + rows : (clip + 1) * padded, :] = zeros
        low_ref[clip * padded + rows : (clip + 1) * padded, :] = zeros


def prepare(place, own, near):
    frames, features = own.shape
    width = features // 4
    padded = -(-frames // LANES) * LANES
    in_spec = pl.BlockSpec((frames, 2 * width), lambda s, *_: (0, s))
    out = jax.ShapeDtypeStruct((2 * padded, features), BF16)
    out_spec = pl.BlockSpec((2 * padded, 2 * width), lambda s, order, place: (0, order[s]))
    order = jnp.stack([place[0] >> 1, 1 - (place[0] >> 1)])
    return call(
        prepare_body,
        grid_spec=pltpu.PrefetchScalarGridSpec(
            num_scalar_prefetch=2,
            grid=(2,),
            in_specs=[in_spec, in_spec],
            out_specs=[out_spec, out_spec],
        ),
        out_shape=[out, out],
        hbm_outs=(0, 1),
        cost_estimate=cost(0, 16 * frames * features),
        name="prepare",
    )(order, place, in_hbm(own), in_hbm(near))


def product(g_high, g_low, x_high, x_low):
    return dot(g_high, x_high, NN) + (dot(g_high, x_low, NN) + dot(g_low, x_high, NN))


def weight_body(turn, place_ref, *refs):
    if turn:
        grad_ref, near_ref, x_high, x_low, kept, sent, g_high, g_low, t_high, t_low = refs

        @pl.when(pl.program_id(0) == 0)
        def _():
            frames, features = grad_ref.shape
            width = features // 4
            rows = width // 4
            padded = t_high.shape[1] // 2
            t_high[...] = jnp.zeros_like(t_high)
            t_low[...] = jnp.zeros_like(t_low)
            for clip in range(2):
                for dh in range(2):
                    if clip == 0:
                        part = grad_ref[:, 2 * dh * width : (2 * dh + 1) * width]
                    else:
                        part = near_ref[:, dh * width : (dh + 1) * width]
                    high, low = split(part.T)
                    at = (
                        slice(dh * width, (dh + 1) * width),
                        slice(clip * padded, clip * padded + frames),
                    )
                    t_high[at] = high
                    t_low[at] = low
            for group in range(8):
                first, second, dh = group // 4, group // 2 % 2, group % 2
                core = place_ref[6]
                y = place_ref[4] ^ (first * core + second * (1 - core))
                x = place_ref[5] ^ (first * (1 - core) + second * core)
                at = pl.multiple_of(dh * width + (2 * y + x) * rows, rows)
                g_high[group * rows : (group + 1) * rows, :] = t_high[pl.ds(at, rows), :]
                g_low[group * rows : (group + 1) * rows, :] = t_low[pl.ds(at, rows), :]

    else:
        g_high, g_low, x_high, x_low, kept, sent = refs
    half = g_high.shape[0] // 2
    value = product(g_high[...], g_low[...], x_high[...], x_low[...])
    kept[...] = value[:half].reshape(kept.shape)
    sent[...] = value[half:].reshape(sent.shape)


def weight_rows(side, place, grads, x_split, width):
    turn = side == 0
    whole = lambda array: pl.BlockSpec(array.shape, lambda s, place: (0,) * array.ndim)
    x_spec = pl.BlockSpec((x_split[0].shape[0], width), lambda s, place: (0, s))
    shape = (2, 2, width // 4, 4 * width)
    out_shape = [jax.ShapeDtypeStruct(shape, F32)] * 2
    out_specs = [pl.BlockSpec(shape[:3] + (width,), lambda s, place: (0, 0, 0, s))] * 2
    scratch = []
    if turn:
        turned = (2 * width, x_split[0].shape[0])
        out_shape += [jax.ShapeDtypeStruct(turned, BF16)] * 2
        out_specs += [whole(out_shape[-1])] * 2
        scratch = [pltpu.VMEM(turned, BF16)] * 2
    return call(
        partial(weight_body, turn),
        grid_spec=pltpu.PrefetchScalarGridSpec(
            num_scalar_prefetch=1,
            grid=(4,),
            in_specs=[whole(a) for a in grads] + [x_spec] * 2,
            out_specs=out_specs,
            scratch_shapes=scratch,
        ),
        out_shape=out_shape,
        hbm_outs=(0,),
        cost_estimate=cost(12 * x_split[0].shape[0] * width * 4 * width, 4 * 8 * width * width),
        name="weight_rows",
    )(place, *([in_hbm(grads[0]), grads[1]] if turn else grads), *[in_hbm(x) for x in x_split])


def step_body(n, widths, cut, *refs):
    ins, outs = refs[: 2 * n], refs[2 * n :]
    starts = [sum(widths[:i]) for i in range(len(widths))]
    column = 0
    for i in range(n):
        total = ins[2 * i][...] + ins[2 * i + 1][...]
        end = column + total.shape[-1]
        for j, (start, columns) in enumerate(zip(starts, widths)):
            low, high = max(start, column), min(start + columns, end)
            if low < high:
                to = (Ellipsis, slice(low - start, high - start))
                piece = total[..., low - column : high - column]
                pieces = [piece]
                for _ in range(cut):
                    pieces = [half[k] for half in pieces for k in range(2)]
                for k, some in enumerate(pieces):
                    outs[len(pieces) * j + k][to] = some
        column = end


def step_of(*pairs, cut=1, widths=None, hbm_outs=()):
    shape = list(pairs[0][0].shape)
    widths = widths or [sum(pair[0].shape[-1] for pair in pairs)]
    outs = []
    for columns in widths:
        shape[-1] = columns
        outs += [jax.ShapeDtypeStruct(tuple(shape[cut:]), F32)] * 2**cut
    whole = lambda array: pl.BlockSpec(array.shape, lambda i: (0,) * array.ndim)
    operands = [array for pair in pairs for array in pair]
    return call(
        partial(step_body, len(pairs), widths, cut),
        grid=(1,),
        in_specs=[whole(a) for a in operands],
        out_specs=[whole(a) for a in outs],
        out_shape=outs,
        hbm_outs=hbm_outs,
        cost_estimate=cost(0, 4 * sum(a.size for a in operands)),
        name="reduction_step",
    )(*operands)


def plane_swap(array, step):
    pairs = []
    for i in range(8):
        over_x = (i % 2 == 0) == (step == 0)
        pairs.append((i, i ^ 2 if over_x else i ^ 4))
    return lax.ppermute(array, ("y", "x", "c"), pairs)


def plane_gather(share, *before):
    first = plane_swap(share, 0)
    second = plane_swap(share, 1)
    return [share, second, first, plane_swap(after(first, second, *before), 1)]


def assemble_body(place_ref, *refs):
    out_ref = refs[-1]
    core = place_ref[6]
    rows, columns = refs[0].shape
    quarter = columns // 4
    for i in range(4):
        first, second = i // 2, i % 2
        y = place_ref[4] ^ (first * core + second * (1 - core))
        x = place_ref[5] ^ (first * (1 - core) + second * core)
        at = pl.multiple_of((2 * y + x) * rows, rows)
        for side in range(2):
            for h in range(2):
                to = pl.multiple_of((2 * h + (place_ref[7] ^ side)) * quarter, quarter)
                some = slice((2 * side + h) * quarter, (2 * side + h + 1) * quarter)
                out_ref[0, pl.ds(at, rows), pl.ds(to, quarter)] = refs[i][:, some]


def assemble(place, pieces, layer, onto=None):
    rows, columns = 4 * pieces[0].shape[0], pieces[0].shape[1]
    aliases, extra, extra_specs = {}, [], []
    if onto is not None:
        aliases, extra = {1 + len(pieces): 0}, [onto]
        extra_specs = [pl.BlockSpec(memory_space=pl.ANY)]
    (out,) = call(
        assemble_body,
        grid=(1,),
        out_shape=[jax.ShapeDtypeStruct((LAYERS, rows, columns), F32)],
        hbm_outs=(0,),
        in_specs=[SMEM_SPEC]
        + [pl.BlockSpec(p.shape, lambda i: (0, 0)) for p in pieces]
        + extra_specs,
        out_specs=[pl.BlockSpec((1, rows, columns), lambda i: (layer, 0, 0))],
        input_output_aliases=aliases,
        cost_estimate=cost(0, 8 * rows * columns),
        name="assemble",
    )(place, *[p if extra else in_hbm(p) for p in pieces], *extra)
    return out


def half_features(inputs, weights, gains, shifts, decays, biases, lengths, frame_mask, grad_out):
    width, slots = inputs.shape
    clips, frames = frame_mask.shape
    depth = weights.shape[2]
    blocks = 4 * width // LANES
    y, x, h, l, c = (lax.axis_index(name) for name in ("y", "x", "h", "l", "c"))
    b = 2 * y + x
    numbers = [2 * (h ^ (rel // 2)) + (c ^ (rel % 2)) for rel in range(4)] + [y, x, c, l]
    place = jnp.stack(numbers).astype(jnp.int32)
    own_blocks, other_blocks = (
        jnp.stack(
            [2 * (2 * (h ^ (rel // 2)) + half) + (c ^ (rel % 2)) for rel in range(4)]
        ).astype(jnp.int32)
        for half in (l, 1 - l)
    )
    own_columns = jnp.stack([2 * h + l, 2 * (1 - h) + l]).astype(jnp.int32)
    other_columns = jnp.stack([2 * (1 - h) + 1 - l, 2 * h + 1 - l]).astype(jnp.int32)
    rows = width // 4

    clip = 2 * h + c
    seen = lax.dynamic_index_in_dim(frame_mask, clip, 0, keepdims=False)
    length = lax.dynamic_index_in_dim(lengths, clip, 0, keepdims=False)
    moments = jnp.arange(frames, dtype=jnp.int32)
    gate = ((moments < length) & ((seen == 1) | (moments == 0))).astype(F32)
    valid = jnp.broadcast_to(gate[:, None], (frames, LANES))

    def far_share(layer):
        return lax.dynamic_slice(weights, (layer, b * rows, 0), (1, rows, depth))[0]

    def over_h(array):
        return lax.ppermute(array, "h", FLIP2)

    def over_c(array):
        return lax.ppermute(array, "c", FLIP2)

    def over_second(array):
        return plane_swap(array, 1)

    def four_of(near_rows, far_rows):
        return [
            (near_rows, 0),
            (over_c(near_rows), 1),
            (far_rows, 0),
            (over_c(far_rows), 1),
        ]

    def four_of_plane(share):
        both = lax.ppermute(share, ("y", "x"), DIAGONAL)
        return [share, lax.ppermute(share, "x", FLIP2), lax.ppermute(share, "y", FLIP2), both]

    near = over_c(weights)
    share = far_share(0)
    close, away = pack(place, after(inputs, share), frames)
    share = over_h(share)
    away = over_h(away)
    other_close = swap_half(close)
    up_close, up_away = pack(place, after(grad_out, close), frames, waits=True)
    share = after(share, up_close, valid, near)
    pieces = four_of_plane(share)
    away = after(away, pieces[1:], other_close)
    half_weights = [[weights, near, *pieces, *map(over_c, after(pieces, away))]]
    own = four_of(after(close, away), away)
    other_away = swap_half(away)
    others = [(other_close, 0), (over_c(other_close), 1)]
    params = jnp.stack([gains, shifts + biases, decays], axis=1)
    own_params = params.reshape(LAYERS * 3 * width // LANES, LANES)
    params = None

    def gather(array, axes):
        return lax.all_gather(array, axes, tiled=True)

    weight = half_weights[0]
    early = jnp.concatenate([own_blocks, other_blocks[:2]])
    z, own_flat = project(place, frames, own + others, early, weight, 0, flat=own)
    others += [(other_away, 0), (over_c(after(other_away, z)[frames:]), 0)]
    z, stats, other_flat = project(
        place,
        frames,
        others[2:],
        other_blocks[2:],
        weight,
        0,
        z,
        valid,
        params=own_params,
        flat=others,
    )
    z = [z]
    stats = gather(stats, ("h", "c"))
    share = over_c(lax.ppermute(after(far_share(1), stats), ("h", "c"), DIAGONAL))
    stats = gather(stats, ("y", "x"))
    x, states, slopes, params = recur(0, place, gate, z, stats, None, valid, own_flat, False)
    own_near, other_near = over_c(after(own_flat, z[0])), over_c(after(other_flat, z[0]))
    x_near = over_c(x)
    own_split = prepare(place, after(own_flat, x_near), own_near)
    other_split = prepare(place, after(other_flat, x_near), other_near)
    saved = [(own_split, other_split, z, stats, states, slopes)]

    pieces = four_of_plane(after(share, slopes, own_near, other_near))
    near = [weights, near]
    other = swap_half(x)
    x_own = after(x, own_split[0], other_split[0])
    z, *_ = project(place, frames, [(x_own, None)], own_blocks, near, 1)
    own_split = prepare(place, after(x, z), x_near)
    far = [*pieces, *map(over_c, after(pieces, own_split[0]))]
    up_away = over_h(after(up_away, own_split[0]))
    half_weights.append(near + far)
    z, stats = project(place, frames, [(other, None)], other_blocks, near, 1, z, valid)
    both = jnp.concatenate([own_blocks, other_blocks])
    z_far, stats = project(
        place,
        frames,
        [(x, None), (other, None)],
        both,
        far,
        1,
        None,
        valid,
        stats,
    )
    z = [z, z_far]
    stats = gather(gather(stats, ("y", "x")), ("h", "c"))
    upstream = four_of(up_close, after(up_away, stats))
    *output, states, slopes = recur(1, place, gate, z, stats, params, valid, x, True)
    other_near = over_c(after(other, slopes))
    saved.append((own_split, (other, other_near), z, stats, states, slopes))
    diagonal = over_c(over_h(output[3]))

    ups = upstream
    results = [None] * LAYERS
    for layer in range(LAYERS - 1, -1, -1):
        own_split, other_split, z, stats, states, slopes = saved[layer]
        weight = half_weights[layer]
        grad_pre, sums = back(layer, place, gate, z, stats, params, ups, states, slopes)
        sums = gather(sums, ("y", "x"))
        if layer == 0:
            come[0] = after(come[0], sums, away, output[1][0])
            later, go = step_of((in_hbm(stay[0]), come[0]), (in_hbm(stay[1]), come[1]))
            sums = after(sums, later)
            go = over_second(go)
        sums = gather(sums, ("h", "c"))
        grad_z, leaving, *terms, sums = norm_back(
            other_columns, place, grad_pre, z, params, valid, stats, sums, weight, layer,
            layer == 0,
        )
        leaving = over_c(leaving)
        if layer > 0:
            received = [swap_half(terms[0])]
            other_split = prepare(place, *after(other_split, grad_z))
            leaving = after(leaving, diagonal, other_split[0])
        else:
            received = [None, swap_half(terms[1])]
            later, go = step_of((later, after(go, grad_z)), hbm_outs=(0,))
            leaving = after(leaving, later)
            go = lax.ppermute(go, ("h", "c"), DIAGONAL)
            later = (later, go)
        *first, g_high, g_low = weight_rows(0, place, (grad_z, leaving), own_split, width)
        turned = (g_high, g_low)
        come = [plane_swap(first[1], 0)]
        if layer == 0:
            received[0] = swap_half(after(terms[0], received[1]))
        second = weight_rows(1, place, turned, other_split, width)
        come.append(plane_swap(second[1], 0))
        stay = (first[0], second[0])
        kept = own_terms(own_columns, place, after(grad_z, second[0]), ups, weight, layer)
        if layer > 0:
            away = over_h(after(output[2], kept))
            output = [(a, 0) for a in (output[0], over_c(output[1]), away, diagonal)]
        ups = [(kept, None)] + [(r, None) for r in received]
        results[layer] = lax.dynamic_index_in_dim(
            sums.reshape(3, 4, width), clip, axis=1, keepdims=False
        )

    sums = jnp.stack(results)
    sums = [sums[:, 0], sums[:, 1], sums[:, 2]]
    aways = merge(kept, 1, received[1], apart=True)
    later = (in_hbm(later[0]), over_c(after(later[1], aways[0])))
    (later,) = step_of(later, cut=0, hbm_outs=(0,))
    come[0] = after(come[0], sums, later)
    far_near = over_c(lax.ppermute(aways[0], ("h", "c"), DIAGONAL))
    near_sum, far_sum, near_go, far_go = step_of(
        (in_hbm(stay[0]), come[0]), (in_hbm(stay[1]), come[1]), cut=2
    )
    near_go, far_go = over_second(near_go), over_second(far_go)
    (go,) = step_of((far_sum, after(far_go, far_near)), cut=0)
    later = after(later, go)
    go = over_h(go)
    later = plane_gather(later)
    (total,) = step_of((near_sum, near_go), cut=0)
    output = unpack(place, [(after(array, total), i) for array, i in output], frames, waited=True)
    close = merge(kept, 0, after(received[0], output))
    far = over_c(over_h(after(aways[1], go)))
    (share,) = step_of((total, after(go, close, *later[1:])), cut=0)
    grad_weights = assemble(place, after(later, share), 1)
    gathered = plane_gather(share, grad_weights)
    grad_in = [(close, 0), (over_c(close[frames:]), 0), (far_near, 0), (far, 0)]
    grad_in = unpack(place, grad_in, frames)
    grad_weights = assemble(place, after(gathered, grad_in), 0, grad_weights)
    return (output, grad_in, grad_weights, *sums, sums[1])


def gelu_slope(value):
    return (
        0.5 * (1.0 + jax.scipy.special.erf(value / ROOT_TWO))
        + value * jnp.exp(-0.5 * value * value) / ROOT_TWO_PI
    )


def recur_step(decay, state, inputs):
    drive_t, valid_t = inputs
    pre = drive_t + decay * state
    state = state + valid_t * (jax.nn.gelu(pre, approximate=False) - state)
    return (state, state)


def back_step(decay, carry, inputs):
    upstream_t, valid_t, pre_t = inputs
    total = upstream_t + carry
    grad_pre = total * valid_t * gelu_slope(pre_t)
    carry = total * (1.0 - valid_t) + grad_pre * decay
    return (carry, grad_pre)


def add_piece(weight, piece):
    return jnp.dot(weight, piece, precision=HIGH, preferred_element_type=jnp.float32)


def weight_columns(grad_pre_norm, piece):
    return jnp.einsum("jf,kf->jk", grad_pre_norm, piece, precision=HIGH)


def split_features(inputs, weights, gains, shifts, decays, biases, lengths, frame_mask, grad_out):
    width, slots = inputs.shape
    clips, frames_len = frame_mask.shape
    frames = jnp.arange(frames_len, dtype=jnp.int32)
    valid_grid = (
        (frames[None, :] < lengths[:, None]) & ((frame_mask == 1) | (frames[None, :] == 0))
    ).astype(jnp.float32)
    valid = valid_grid.reshape(-1)
    valid_row = valid[None, :]
    valid_time = jnp.broadcast_to(valid_grid.T[:, :, None], (frames_len, clips, width)).reshape(
        frames_len, clips * width
    )
    count_local = jnp.sum(valid)

    def to_time(array):
        return jnp.transpose(array.reshape(width, clips, frames_len), (2, 1, 0)).reshape(
            frames_len, clips * width
        )

    def from_time(array):
        return jnp.transpose(array.reshape(frames_len, clips, width), (2, 1, 0)).reshape(
            width, slots
        )

    layer_in = inputs
    saved = []
    for layer_no in range(LAYERS):
        weight = weights[layer_no]
        gathered = lax.all_gather(layer_in, "neuron", axis=0, tiled=True)
        pre_norm = add_piece(weight, gathered)
        first_sum, count = lax.psum((jnp.sum(valid_row * pre_norm, axis=1), count_local), "batch")
        mean = first_sum / count
        centered = pre_norm - mean[:, None]
        var = lax.psum(jnp.sum(valid_row * centered * centered, axis=1), "batch") / count
        inv_std = lax.rsqrt(var + EPS)
        zhat = (pre_norm - mean[:, None]) * inv_std[:, None]
        drive = gains[layer_no][:, None] * zhat + (shifts[layer_no] + biases[layer_no])[:, None]
        drive_time = to_time(drive)
        decay_wide = jnp.tile(decays[layer_no], clips)
        start_state = jnp.zeros((clips * width,), jnp.float32)
        _, states = lax.scan(
            partial(recur_step, decay_wide), start_state, (drive_time, valid_time), unroll=8
        )
        saved.append((gathered, zhat, inv_std, drive_time, states, count))
        layer_in = layer_in + valid_row * from_time(states)
    upstream = grad_out
    grad_parts = [None] * LAYERS
    for layer_no in range(LAYERS - 1, -1, -1):
        gathered, zhat, inv_std, drive_time, states, count = saved[layer_no]
        decay_wide = jnp.tile(decays[layer_no], clips)
        gain = gains[layer_no]
        previous = jnp.concatenate([jnp.zeros_like(states[:1]), states[:-1]], axis=0)
        pre_time = drive_time + decay_wide[None, :] * previous
        grad_state = to_time(valid_row * upstream)
        start_carry = jnp.zeros((clips * width,), jnp.float32)
        _, grad_pre_time = lax.scan(
            partial(back_step, decay_wide),
            start_carry,
            (grad_state, valid_time, pre_time),
            reverse=True,
            unroll=8,
        )
        decay_local = jnp.sum(
            jnp.sum(grad_pre_time * previous, axis=0).reshape(clips, width), axis=0
        )
        grad_pre = from_time(grad_pre_time)
        gain_local = jnp.sum(grad_pre * zhat, axis=1)
        shift_local = jnp.sum(grad_pre, axis=1)
        grad_gain, grad_shift, grad_decay = lax.psum(
            (gain_local, shift_local, decay_local), "batch"
        )
        grad_pre_norm = (gain * inv_std)[:, None] * (
            grad_pre - valid_row * (grad_shift[:, None] + zhat * grad_gain[:, None]) / count
        )
        weight_local = weight_columns(grad_pre_norm, gathered)
        input_terms = jnp.einsum("jk,jf->kf", weights[layer_no], grad_pre_norm, precision=HIGH)
        input_grad = lax.psum_scatter(input_terms, "neuron", scatter_dimension=0, tiled=True)
        grad_weight = lax.psum(weight_local, "batch")
        upstream = upstream + input_grad
        grad_parts[layer_no] = (grad_weight, grad_gain, grad_shift, grad_decay)
    grad_weights = jnp.stack([grad_parts[layer_no][0] for layer_no in range(LAYERS)])
    grad_gains = jnp.stack([grad_parts[layer_no][1] for layer_no in range(LAYERS)])
    grad_shifts = jnp.stack([grad_parts[layer_no][2] for layer_no in range(LAYERS)])
    grad_decays = jnp.stack([grad_parts[layer_no][3] for layer_no in range(LAYERS)])
    return (layer_in, upstream, grad_weights, grad_gains, grad_shifts, grad_decays, grad_shifts)


def solution(mesh):
    if (mesh.shape["batch"], mesh.shape["neuron"]) == (4, 8):
        cut = Mesh(mesh.devices.reshape(2, 2, 2, 2, 2), ("y", "x", "h", "l", "c"))
        batch, neuron, body = ("y", "x"), ("h", "l", "c"), half_features
    else:
        cut, batch, neuron, body = mesh, "batch", "neuron", split_features
    in_specs = (
        P(neuron, batch),
        P(None, neuron, None),
        P(None, neuron),
        P(None, neuron),
        P(None, neuron),
        P(None, neuron),
        P(batch),
        P(batch, None),
        P(neuron, batch),
    )
    out_specs = (
        P(neuron, batch),
        P(neuron, batch),
        P(None, neuron, None),
        P(None, neuron),
        P(None, neuron),
        P(None, neuron),
        P(None, neuron),
    )
    return jax.shard_map(
        body, mesh=cut, in_specs=in_specs, out_specs=out_specs, check_vma=False
    )
```

```python
from functools import partial
import math

import jax
import jax.numpy as jnp
from jax import lax
from jax.experimental import pallas as pl
from jax.experimental.pallas import tpu as pltpu
from jax.sharding import Mesh, PartitionSpec as P

LAYERS = 2
EPS = 1e-05
HIGH = lax.Precision.HIGHEST
ROOT_TWO = math.sqrt(2.0)
ROOT_TWO_PI = math.sqrt(2.0 * math.pi)
F32 = jnp.float32
BF16 = jnp.bfloat16
LANES = 128
VMEM_LIMIT = 24 * 1024 * 1024
SMEM_SPEC = pl.BlockSpec(memory_space=pltpu.SMEM)
VMEM_SPEC = pl.BlockSpec(memory_space=pltpu.VMEM)


FLIP2 = [(0, 1), (1, 0)]
DIAGONAL = [(0, 3), (1, 2), (2, 1), (3, 0)]


def swap_half(array):
    return lax.ppermute(array, "l", FLIP2)


def after(value, *others):
    return lax.optimization_barrier((value, others))[0]


def split(value):
    high = value.astype(BF16)
    return high, (value - high.astype(F32)).astype(BF16)


def dot(a, b, dims):
    return lax.dot_general(a, b, (dims, ((), ())), preferred_element_type=F32)


NT = ((1,), (1,))
NN = ((1,), (0,))


def in_hbm(array):
    return pltpu.with_memory_space_constraint(array, pltpu.HBM)


def call(body, out_shape, hbm_outs=(), **kwargs):
    if hbm_outs:
        out_shape = [
            pltpu.HBM(a.shape, a.dtype) if i in hbm_outs else a for i, a in enumerate(out_shape)
        ]
    return pl.pallas_call(
        body,
        out_shape=out_shape,
        compiler_params=pltpu.CompilerParams(vmem_limit_bytes=VMEM_LIMIT),
        **kwargs,
    )


def cost(flops, byte_count):
    return pl.CostEstimate(flops=int(flops) // 64, bytes_accessed=int(byte_count) // 64, transcendentals=0)


def pack_body(frames, place_ref, in_ref, near_ref, far_ref, turned):
    slots = in_ref.shape[1]
    for start in range(0, slots, LANES):
        turned[start : start + LANES, :] = in_ref[:, start : start + LANES].T
    for rel in range(4):
        first = pl.multiple_of(place_ref[rel] * frames, 8)
        out = (near_ref, far_ref)[rel // 2]
        out[(rel % 2) * frames : (rel % 2 + 1) * frames, :] = turned[pl.ds(first, frames), :]


def pack(place, array, frames, waits=False):
    width, slots = array.shape
    out = jax.ShapeDtypeStruct((2 * frames, width), F32)
    return call(
        partial(pack_body, frames),
        grid=(1,),
        out_shape=[out, out],
        in_specs=[SMEM_SPEC, pl.BlockSpec((width, slots), lambda i: (0, 0))],
        out_specs=[pl.BlockSpec(out.shape, lambda i: (0, 0))] * 2,
        scratch_shapes=[pltpu.VMEM((slots, width), F32)],
        hbm_outs=(0, 1) if waits else (),
        cost_estimate=cost(0, 8 * width * slots),
        name="pack",
    )(place, in_hbm(array))


def part_spec(part, frames):
    array, i = part
    if i is None:
        return pl.BlockSpec(array.shape, lambda *_: (0,) * array.ndim)
    return pl.BlockSpec((frames, array.shape[1]), lambda *_: (i, 0))


def arrays_of(parts):
    return [array for array, _ in parts]


def unpack_body(frames, place_ref, *refs):
    ins, out_ref, turned = refs[:4], refs[4], refs[5]
    slots = out_ref.shape[1]
    for rel in range(4):
        first = pl.multiple_of(place_ref[rel] * frames, 8)
        turned[pl.ds(first, frames), :] = ins[rel][...]
    for start in range(0, slots, LANES):
        out_ref[:, start : start + LANES] = turned[start : start + LANES, :].T


def unpack(place, parts, frames, waited=False):
    width = parts[0][0].shape[1]
    slots = 4 * frames
    return call(
        partial(unpack_body, frames),
        grid=(1,),
        out_shape=jax.ShapeDtypeStruct((width, slots), F32),
        in_specs=[SMEM_SPEC] + [part_spec(part, frames) for part in parts],
        out_specs=pl.BlockSpec((width, slots), lambda i: (0, 0)),
        scratch_shapes=[pltpu.VMEM((slots, width), F32)],
        cost_estimate=cost(0, 8 * width * slots),
        name="unpack",
    )(place, *[in_hbm(a) if waited else a for a in arrays_of(parts)])


def merge_body(kept_ref, come_ref, *outs):
    frames, columns = kept_ref.shape
    width = columns // 2
    for i in range(2):
        some = slice(i * width, (i + 1) * width)
        if len(outs) > 1:
            outs[i][...] = kept_ref[:, some] + come_ref[:, some]
            continue
        (out_ref,) = outs
        out_ref[i * frames : (i + 1) * frames, :] = kept_ref[:, some] + come_ref[:, some]


def merge(kept, half, come, apart=False):
    frames, columns = come.shape
    rows, n = (frames, 2) if apart else (2 * frames, 1)
    outs = call(
        merge_body,
        hbm_outs=(0, 1) if apart else (),
        grid=(1,),
        out_shape=[jax.ShapeDtypeStruct((rows, columns // 2), F32)] * n,
        in_specs=[
            pl.BlockSpec((frames, columns), lambda i: (0, half)),
            pl.BlockSpec((frames, columns), lambda i: (0, 0)),
        ],
        out_specs=[pl.BlockSpec((rows, columns // 2), lambda i: (0, 0))] * n,
        cost_estimate=cost(0, 12 * frames * columns),
        name="merge",
    )(kept, come)
    return outs if apart else outs[0]


def project_body(n_parts, n_flat, spots, n_weights, first, with_acc, with_stats, with_params, cols_ref, place_ref, *refs):
    del cols_ref

    def take(n):
        nonlocal refs
        some, refs = refs[:n], refs[n:]
        return some

    parts, flat_parts, weights = take(n_parts), take(n_flat), take(n_weights)
    acc, valid, stats_in, params = take(with_acc), take(with_stats > 0), take(with_stats > 1), take(with_params)
    (out_ref,) = take(1)
    stats, flat = take(with_stats > 0), take(n_flat > 0)
    x_high, x_low, far_ref = refs
    step = pl.program_id(0)
    width = x_high.shape[2]

    @pl.when(step == 0)
    def _():
        for block, part in zip(spots, parts):
            for start in range(0, part.shape[1], width):
                high, low = split(part[:, start : start + width])
                x_high[block + start // width] = high
                x_low[block + start // width] = low
        column = 0
        for part in flat_parts:
            flat[0][:, column : column + part.shape[1]] = part[...]
            column += part.shape[1]
        if with_acc:
            out_ref[...] = acc[0][...]
        else:
            out_ref[...] = jnp.zeros_like(out_ref)

    stacked = jnp.concatenate([x_high[step], x_low[step], x_high[step]], axis=1)
    for block, weight in enumerate(weight_blocks(place_ref, weights, far_ref)):
        w_high, w_low = split(weight)
        columns = slice(block * width, (block + 1) * width)
        out_ref[:, columns] += dot(stacked, jnp.concatenate([w_high, w_high, w_low], axis=1), NT)

    if with_stats:
        (stats_ref,) = stats

        @pl.when(step == pl.num_programs(0) - 1)
        def _():
            if stats_in:
                stats_ref[...] = stats_in[0][...]
            own = jnp.sum(valid[0][...], axis=0, keepdims=True)
            per = width // LANES
            for row in range(out_ref.shape[1] // LANES):
                z = out_ref[:, row * LANES : (row + 1) * LANES]
                total = jnp.sum(valid[0][...] * z, axis=0, keepdims=True)
                centred = valid[0][...] * (z - total / own)
                squares = jnp.sum(centred * centred, axis=0, keepdims=True)
                at = place_ref[first + row // per] * per + row % per
                stats_ref[0, pl.ds(at, 1), :] = total
                stats_ref[1, pl.ds(at, 1), :] = squares
                stats_ref[2, pl.ds(at, 1), :] = own
            if with_params:
                rest = params[0].shape[0] - 8
                stats_ref[3] = params[0][:8, :]
                stats_ref[4] = jnp.zeros_like(stats_ref[4])
                stats_ref[4, :rest, :] = params[0][8:, :]


def weight_specs(weights, layer, pairs=2):
    specs = []
    for weight in weights:
        if weight.ndim == 3:
            shape = (1, weight.shape[1], pairs * weight.shape[1])
            specs.append(pl.BlockSpec(shape, lambda s, cols, *_: (layer, 0, cols[s])))
        else:
            shape = (weight.shape[0], pairs * 4 * weight.shape[0])
            specs.append(pl.BlockSpec(shape, lambda s, cols, *_: (0, cols[s])))
    return specs


def far_scratch(width, pairs=2):
    return pltpu.VMEM((2, width, pairs * width), F32)


def weight_blocks(place_ref, refs, far_ref):
    near = [ref[0] for ref in refs if len(ref.shape) == 3]
    pieces = [ref for ref in refs if len(ref.shape) == 2]
    far = []
    for i in range(len(pieces) // 4):
        for rel, piece in enumerate(pieces[4 * i : 4 * i + 4]):
            rows = piece.shape[0]
            row = 2 * (place_ref[4] ^ (rel // 2)) + (place_ref[5] ^ (rel % 2))
            far_ref[i, pl.ds(pl.multiple_of(row * rows, rows), rows), :] = piece[...]
        far.append(far_ref[i])
    return near + far


def project(
    place, frames, parts, blocks, weights, layer, acc=None, valid=None, stats=None, params=None, flat=()
):
    near = weights[0].ndim == 3
    units = sum(1 if w.ndim == 3 else 0.25 for w in weights)
    width = weights[0].shape[1] if near else 4 * weights[0].shape[0]
    n = blocks.shape[0]
    spots, block = [], 0
    for array, _ in parts:
        spots.append(block)
        block += array.shape[1] // width
    full = pl.BlockSpec(memory_space=pltpu.VMEM)
    in_specs = [part_spec(part, frames) for part in (*parts, *flat)]
    in_specs += weight_specs(weights, layer, 1)
    operands = arrays_of(parts) + arrays_of(flat) + [in_hbm(w) for w in weights]
    array = jax.ShapeDtypeStruct((frames, int(units) * width), F32)
    array_spec = pl.BlockSpec(array.shape, lambda s, cols, place: (0, 0))
    out_shape, out_specs = [array], [array_spec]
    if acc is not None:
        in_specs.append(array_spec)
        operands.append(in_hbm(acc))
    if valid is not None:
        in_specs.append(full)
        operands.append(valid)
        shape = (3 if params is None else 5, 4 * width // LANES, LANES)
        out_shape.append(jax.ShapeDtypeStruct(shape, F32))
        out_specs.append(pl.BlockSpec(shape, lambda s, cols, place: (0, 0, 0)))
    for extra in (stats, params):
        if extra is not None:
            in_specs.append(full)
            operands.append(extra)
    if flat:
        out_shape.append(jax.ShapeDtypeStruct((frames, 4 * width), F32))
        out_specs.append(pl.BlockSpec((frames, 4 * width), lambda s, cols, place: (0, 0)))
    return call(
        partial(
            project_body,
            len(parts),
            len(flat),
            spots,
            len(weights),
            0 if near else 2,
            acc is not None,
            (valid is not None) + (stats is not None),
            params is not None,
        ),
        grid_spec=pltpu.PrefetchScalarGridSpec(
            num_scalar_prefetch=2,
            grid=(n,),
            in_specs=in_specs,
            out_specs=out_specs,
            scratch_shapes=[pltpu.VMEM((n, frames, width), BF16)] * 2 + [far_scratch(width, 1)],
        ),
        out_shape=out_shape,
        hbm_outs=(0, len(out_shape) - 1) if flat else (0,),
        cost_estimate=cost(6 * frames * n * width * units * width, 4 * n * width * units * width),
        name="project",
    )(blocks, place, *operands)


def to_relative(place_ref, spread, rows_ref, value, slot):
    per = value.shape[0] // 4
    spread[...] = value
    for rel in range(4):
        first = place_ref[rel] * per
        for row in range(per):
            rows_ref[slot, rel * per + row : rel * per + row + 1, :] = spread[
                pl.ds(first + row, 1), :
            ]


def tree(values):
    while len(values) > 1:
        values = [a + b for a, b in zip(values[::2], values[1::2])]
    return values[0]


def gathered(ref, slot):
    return [ref[i] for i in range(slot, ref.shape[0], ref.shape[0] // 16)]


def norm_terms(stats_ref):
    each = [gathered(stats_ref, slot) for slot in range(3)]
    totals, squares, owns = each
    count = tree(owns)
    mean = tree(totals) / count
    away = [total / own - mean for total, own in zip(totals, owns)]
    spread = tree([s + n * a * a for s, n, a in zip(squares, owns, away)])
    return count, mean, lax.rsqrt(spread / count + EPS)


CHUNKS = 4


def columns_of(refs, row):
    for ref in refs:
        if row * LANES < ref.shape[1]:
            return ref[:, row * LANES : (row + 1) * LANES]
        row -= ref.shape[1] // LANES


def recur_body(n_z, last, layer, spread_params, place_ref, gate_ref, *refs):
    z_refs, refs = refs[:n_z], refs[n_z:]
    (stats_ref, params_ref, valid_ref, x_ref), refs = refs[:4], refs[4:]
    outs, refs = refs[: 1 + 3 * last], refs[1 + 3 * last :]
    if spread_params:
        state_ref, slope_ref, params_out, rows, spread, held, drive_s, state_s, slope_s = refs
    else:
        state_ref, slope_ref, rows, spread, held, drive_s, state_s, slope_s = refs
    frames, features = x_ref.shape
    blocks = features // LANES
    per = blocks // 4
    chunk = pl.program_id(0)

    @pl.when(chunk == 0)
    def _():
        if spread_params:
            for rel in range(4):
                first = place_ref[rel] * (stats_ref.shape[0] // 16) + 3
                for row in range(LAYERS * 3 * per):
                    at = rel * per + row % per
                    params_out[row // per, at : at + 1, :] = stats_ref[
                        first + row // 8, row % 8 : row % 8 + 1, :
                    ]
            params = [params_out[3 * layer + i] for i in range(3)]
        else:
            params = [params_ref[3 * layer + i] for i in range(3)]
        _, mean, inv_std = norm_terms(stats_ref)
        to_relative(place_ref, spread, rows, mean, 0)
        to_relative(place_ref, spread, rows, inv_std, 1)
        rows[1] = rows[1] * params[0]
        rows[2] = params[1]
        rows[3] = params[2]
        held[...] = jnp.zeros_like(held)

    for row in range(blocks):
        drive_s[row * frames : (row + 1) * frames, :] = (
            columns_of(z_refs, row) - rows[0, row : row + 1, :]
        ) * rows[1, row : row + 1, :] + rows[2, row : row + 1, :]
    decay = rows[3]

    def step(t, state):
        at = pl.ds(t, blocks, stride=frames)
        pre = drive_s[at, :] + decay * state
        half = 0.5 + 0.5 * lax.erf(pre * (1.0 / ROOT_TWO))
        gate = gate_ref[chunk * frames + t] > 0.0
        slope = half + pre * jnp.exp(-0.5 * pre * pre) * (1.0 / ROOT_TWO_PI)
        state = jnp.where(gate, pre * half, state)
        state_s[at, :] = state
        slope_s[at, :] = jnp.where(gate, slope, 0.0)
        return state

    held[...] = lax.fori_loop(0, frames, step, held[...], unroll=8)
    valid = valid_ref[...]
    for row in range(blocks):
        lanes = slice(row * LANES, (row + 1) * LANES)
        state = state_s[row * frames : (row + 1) * frames, :]
        state_ref[:, lanes] = state
        slope_ref[:, lanes] = slope_s[row * frames : (row + 1) * frames, :]
        value = x_ref[:, lanes] + valid * state
        out, at = (outs[row // per], row % per) if last else (outs[0], row)
        out[:, at * LANES : (at + 1) * LANES] = value


def recur(layer, place, gate, z, stats, params, valid, x, last):
    frames, features = x.shape
    blocks = features // LANES
    some = frames // CHUNKS
    whole = lambda array: pl.BlockSpec(array.shape, lambda i: (0,) * array.ndim)
    by_chunk = lambda array: pl.BlockSpec((some, array.shape[1]), lambda i: (i, 0))
    full = jax.ShapeDtypeStruct((frames, features), F32)
    piece = jax.ShapeDtypeStruct((frames, features // 4), F32)
    out_shape = [piece] * 4 if last else [full]
    out_shape += [full, full]
    out_specs = [by_chunk(a) for a in out_shape]
    spread_params = params is None
    if spread_params:
        out_shape.append(jax.ShapeDtypeStruct((3 * LAYERS, blocks, LANES), F32))
        out_specs.append(whole(out_shape[-1]))
        params = valid
    return call(
        partial(recur_body, len(z), last, layer, spread_params),
        grid=(CHUNKS,),
        in_specs=[SMEM_SPEC, SMEM_SPEC]
        + [by_chunk(a) for a in z]
        + [whole(a) for a in (stats, params)]
        + [by_chunk(a) for a in (valid, x)],
        out_specs=out_specs,
        out_shape=out_shape,
        hbm_outs=tuple(range(len(out_shape) - spread_params)) if last else (1, 2),
        scratch_shapes=[
            pltpu.VMEM((4, blocks, LANES), F32),
            pltpu.VMEM((blocks, LANES), F32),
            pltpu.VMEM((blocks, LANES), F32),
        ]
        + [pltpu.VMEM((blocks * some, LANES), F32)] * 3,
        cost_estimate=cost(100 * frames * features, 20 * frames * features),
        name="recur",
    )(place, gate, *[in_hbm(a) for a in z], stats, params, valid, in_hbm(x))


def back_body(n_z, n_ups, spots, layer, place_ref, gate_ref, *refs):
    z_refs, refs = refs[:n_z], refs[n_z:]
    (stats_ref, params_ref), refs = refs[:2], refs[2:]
    ups, (state_ref, slope_ref), refs = refs[:n_ups], refs[n_ups : n_ups + 2], refs[n_ups + 2 :]
    grad_ref, sums_ref, rows, spread, held, up_s, state_s, slope_s = refs
    frames, features = state_ref.shape
    blocks = features // LANES
    per = blocks // 4
    tall = frames + 8
    step_no = pl.program_id(0)
    chunk = pl.num_programs(0) - 1 - step_no

    @pl.when(step_no == 0)
    def _():
        _, mean, inv_std = norm_terms(stats_ref)
        to_relative(place_ref, spread, rows, mean, 0)
        to_relative(place_ref, spread, rows, inv_std, 1)
        held[...] = jnp.zeros_like(held)

    for row in range(blocks):
        lanes = slice(row * LANES, (row + 1) * LANES)
        base = row * frames
        up = None
        for (_, column), part in zip(spots, ups):
            if column <= row * LANES < column + part.shape[1]:
                value = part[:, row * LANES - column : (row + 1) * LANES - column]
                up = value if up is None else up + value
        up_s[base : base + frames, :] = up
        state_s[row * tall : row * tall + 8, :] = jnp.zeros((8, LANES), F32)
        state_s[row * tall + 8 : (row + 1) * tall, :] = state_ref[:, lanes]
        slope_s[base : base + frames, :] = slope_ref[:, lanes]
    decay = params_ref[3 * layer + 2]

    def step(i, carry):
        t = frames - 1 - i
        at = pl.ds(t, blocks, stride=frames)
        slope = slope_s[at, :]
        gate = gate_ref[chunk * frames + t]
        total = gate * up_s[at, :] + carry
        up_s[at, :] = total * slope
        return total * (slope * decay + (1.0 - gate))

    held[0] = lax.fori_loop(0, frames, step, held[0], unroll=8)
    held[4] += held[1] * state_s[pl.ds(tall - 1, blocks, stride=tall), :]
    held[1] = up_s[pl.ds(0, blocks, stride=frames), :]
    for row in range(blocks):
        lanes = slice(row * LANES, (row + 1) * LANES)
        grad = up_s[row * frames : (row + 1) * frames, :]
        grad_ref[:, lanes] = grad
        zhat = (columns_of(z_refs, row) - rows[0, row : row + 1, :]) * rows[1, row : row + 1, :]
        before = state_s[row * tall + 7 : row * tall + 7 + frames, :]
        for slot, value in enumerate((grad * zhat, grad, grad * before)):
            held[2 + slot, row : row + 1, :] += jnp.sum(value, axis=0, keepdims=True)

    @pl.when(chunk == 0)
    def _():
        for row in range(blocks):
            at = place_ref[row // per] * per + row % per
            for slot in range(3):
                sums_ref[slot, pl.ds(at, 1), :] = held[2 + slot, row : row + 1, :]


def spots_of_sum(parts, width):
    spots, column = [], 0
    for array, _ in parts:
        spots.append((0, column % (4 * width)))
        column += array.shape[1]
    return spots


def back(layer, place, gate, z, stats, params, ups, states, slopes):
    frames, features = states.shape
    width = features // 4
    blocks = features // LANES
    some = frames // CHUNKS
    whole = lambda array: pl.BlockSpec(array.shape, lambda i: (0,) * array.ndim)

    def by_chunk(array, first=0):
        return pl.BlockSpec(
            (some, array.shape[1]), lambda i: ((first or 0) * CHUNKS + CHUNKS - 1 - i, 0)
        )

    out_shape = [
        jax.ShapeDtypeStruct((frames, features), F32),
        jax.ShapeDtypeStruct((3, blocks, LANES), F32),
    ]
    return call(
        partial(back_body, len(z), len(ups), spots_of_sum(ups, width), layer),
        grid=(CHUNKS,),
        in_specs=[SMEM_SPEC] * 2
        + [by_chunk(a) for a in z]
        + [whole(a) for a in (stats, params)]
        + [by_chunk(*up) for up in ups]
        + [by_chunk(a) for a in (states, slopes)],
        out_specs=[by_chunk(out_shape[0]), whole(out_shape[1])],
        out_shape=out_shape,
        scratch_shapes=[
            pltpu.VMEM((2, blocks, LANES), F32),
            pltpu.VMEM((blocks, LANES), F32),
            pltpu.VMEM((5, blocks, LANES), F32),
            pltpu.VMEM((blocks * some, LANES), F32),
            pltpu.VMEM((blocks * (some + 8), LANES), F32),
            pltpu.VMEM((blocks * some, LANES), F32),
        ],
        cost_estimate=cost(30 * frames * features, 20 * frames * features),
        name="back",
    )(
        place,
        gate,
        *[in_hbm(a) for a in z],
        stats,
        params,
        *arrays_of(ups),
        in_hbm(states),
        in_hbm(slopes),
    )


def input_terms(high_s, low_s, weights):
    left, right = [], []
    for block, weight in enumerate(weights):
        w_high, w_low = split(weight)
        left += [high_s[block], low_s[block], high_s[block]]
        right += [w_high, w_high, w_low]
    return dot(jnp.concatenate(left, axis=1), jnp.concatenate(right, axis=0), NN)


def norm_back_body(n_z, split_terms, layer, cols_ref, place_ref, grad_ref, *refs):
    del cols_ref
    z_refs, refs = refs[:n_z], refs[n_z:]
    params_ref, valid_ref, stats_ref, sums_ref, *refs = refs
    weights, refs = refs[:10], refs[10:]
    if split_terms:
        out_ref, leave_ref, near_term_ref, far_term_ref, sums_out_ref, *refs = refs
        term_refs, starts = (far_term_ref, near_term_ref), (0, 0)
    else:
        out_ref, leave_ref, term_ref, sums_out_ref, *refs = refs
        term_refs, starts = (term_ref, term_ref), (2 * grad_ref.shape[1] // 4, 0)
    rows, spread, high_s, low_s, far_ref = refs
    blocks = grad_ref.shape[1] // LANES
    width = high_s.shape[2]
    per = width // LANES

    @pl.when(pl.program_id(0) == 0)
    def _():
        count, mean, inv_std = norm_terms(stats_ref)
        to_relative(place_ref, spread, rows, mean, 0)
        to_relative(place_ref, spread, rows, inv_std, 1)
        rows[2] = rows[1] * params_ref[3 * layer]
        sums = [tree(gathered(sums_ref, slot)) for slot in range(3)]
        for slot in range(3):
            sums_out_ref[slot] = sums[slot]
        to_relative(place_ref, spread, rows, sums[0] / count, 3)
        to_relative(place_ref, spread, rows, sums[1] / count, 4)
        valid = valid_ref[...]
        for row in range(blocks):
            lanes = slice(row * LANES, (row + 1) * LANES)
            one = lambda slot: rows[slot, row : row + 1, :]
            zhat = (columns_of(z_refs, row) - one(0)) * one(1)
            value = one(2) * (grad_ref[:, lanes] - valid * (one(4) + zhat * one(3)))
            out_ref[:, lanes] = value
            if (row // per) % 2:
                at = (row // per // 2) * width + (row % per) * LANES
                leave_ref[:, at : at + LANES] = value
            high, low = split(value)
            inner = slice((row % per) * LANES, (row % per + 1) * LANES)
            high_s[row // per, :, inner] = high
            low_s[row // per, :, inner] = low

    value = input_terms(high_s, low_s, weight_blocks(place_ref, weights, far_ref))
    for step, (term_ref, first) in enumerate(zip(term_refs, starts)):

        @pl.when(pl.program_id(0) == step)
        def _():
            for pair in range(2):
                at = pl.multiple_of(((place_ref[0] & 1) ^ pair) * width, width)
                term_ref[:, pl.ds(first + at, width)] = value[
                    :, pair * width : (pair + 1) * width
                ]


def norm_back(columns, place, grad, z, params, valid, stats, sums, weights, layer, split_terms):
    frames, features = grad.shape
    width = features // 4
    blocks = features // LANES
    whole = lambda array: pl.BlockSpec(array.shape, lambda s, cols, place: (0,) * array.ndim)
    operands = [grad, *[in_hbm(a) for a in z], params, valid, stats, sums]
    full = jax.ShapeDtypeStruct((frames, features), F32)
    half = jax.ShapeDtypeStruct((frames, 2 * width), F32)
    terms = [half, half] if split_terms else [full]
    out_shape = [full, half, *terms, jax.ShapeDtypeStruct((3, blocks, LANES), F32)]
    return call(
        partial(norm_back_body, len(z), split_terms, layer),
        grid_spec=pltpu.PrefetchScalarGridSpec(
            num_scalar_prefetch=2,
            grid=(2,),
            in_specs=[whole(a) for a in operands] + weight_specs(weights, layer),
            out_specs=[whole(a) for a in out_shape],
            scratch_shapes=[
                pltpu.VMEM((5, blocks, LANES), F32),
                pltpu.VMEM((blocks, LANES), F32),
                pltpu.VMEM((4, frames, width), BF16),
                pltpu.VMEM((4, frames, width), BF16),
                far_scratch(width),
            ],
        ),
        out_shape=out_shape,
        hbm_outs=(0, 2) if split_terms else (0,),
        cost_estimate=cost(6 * frames * features * features, 4 * features * features),
        name="norm_back",
    )(columns, place, *operands, *[in_hbm(w) for w in weights])


def own_terms_body(n_ups, spots, cols_ref, place_ref, grad_ref, *refs):
    del cols_ref
    ups, refs = refs[:n_ups], refs[n_ups:]
    weights, refs = refs[:10], refs[10:]
    out_ref, high_s, low_s, far_ref = refs
    width = high_s.shape[2]
    step = pl.program_id(0)

    @pl.when(step == 0)
    def _():
        for block in range(4):
            high, low = split(grad_ref[:, block * width : (block + 1) * width])
            high_s[block] = high
            low_s[block] = low

    value = input_terms(high_s, low_s, weight_blocks(place_ref, weights, far_ref))
    for pair in range(2):
        at = pl.multiple_of(((place_ref[0] & 1) ^ pair) * width, width)
        out_ref[:, pl.ds(at, width)] = value[:, pair * width : (pair + 1) * width]
    for half in range(2):

        @pl.when(step == half)
        def _():
            first = 2 * half * width
            for (_, column), up in zip(spots, ups):
                low = max(column, first)
                high = min(column + up.shape[1], first + 2 * width)
                if low < high:
                    out_ref[:, low - first : high - first] += up[:, low - column : high - column]


def own_terms(columns, place, grad, ups, weights, layer):
    frames, features = grad.shape
    width = features // 4
    whole = lambda array: pl.BlockSpec(array.shape, lambda s, cols, place: (0,) * array.ndim)
    step_block = pl.BlockSpec((frames, 2 * width), lambda s, cols, place: (0, s))
    return call(
        partial(own_terms_body, len(ups), spots_of_sum(ups, width)),
        grid_spec=pltpu.PrefetchScalarGridSpec(
            num_scalar_prefetch=2,
            grid=(2,),
            in_specs=[whole(grad)]
            + [part_spec(up, frames) for up in ups]
            + weight_specs(weights, layer),
            out_specs=step_block,
            scratch_shapes=[pltpu.VMEM((4, frames, width), BF16)] * 2 + [far_scratch(width)],
        ),
        out_shape=jax.ShapeDtypeStruct((frames, features), F32),
        cost_estimate=cost(6 * frames * features * features, 4 * features * features),
        name="own_terms",
    )(columns, place, in_hbm(grad), *arrays_of(ups), *[in_hbm(w) for w in weights])


def prepare_body(lists_ref, place_ref, own_ref, near_ref, high_ref, low_ref):
    del lists_ref
    padded = high_ref.shape[0] // 2
    width = high_ref.shape[1] // 2
    for clip, part in enumerate((own_ref, near_ref)):
        rows = part.shape[0]
        for dc in range(2):
            at = pl.multiple_of((place_ref[6] ^ clip ^ dc) * width, width)
            high, low = split(part[:, dc * width : (dc + 1) * width])
            high_ref[clip * padded : clip * padded + rows, pl.ds(at, width)] = high
            low_ref[clip * padded : clip * padded + rows, pl.ds(at, width)] = low
        zeros = jnp.zeros((padded - rows, 2 * width), BF16)
        high_ref[clip * padded + rows : (clip + 1) * padded, :] = zeros
        low_ref[clip * padded + rows : (clip + 1) * padded, :] = zeros


def prepare(place, own, near):
    frames, features = own.shape
    width = features // 4
    padded = -(-frames // LANES) * LANES
    in_spec = pl.BlockSpec((frames, 2 * width), lambda s, *_: (0, s))
    out = jax.ShapeDtypeStruct((2 * padded, features), BF16)
    out_spec = pl.BlockSpec((2 * padded, 2 * width), lambda s, order, place: (0, order[s]))
    order = jnp.stack([place[0] >> 1, 1 - (place[0] >> 1)])
    return call(
        prepare_body,
        grid_spec=pltpu.PrefetchScalarGridSpec(
            num_scalar_prefetch=2,
            grid=(2,),
            in_specs=[in_spec, in_spec],
            out_specs=[out_spec, out_spec],
        ),
        out_shape=[out, out],
        hbm_outs=(0, 1),
        cost_estimate=cost(0, 16 * frames * features),
        name="prepare",
    )(order, place, in_hbm(own), in_hbm(near))


def product(g_high, g_low, x_high, x_low):
    return dot(g_high, x_high, NN) + (dot(g_high, x_low, NN) + dot(g_low, x_high, NN))


def weight_body(turn, place_ref, *refs):
    if turn:
        grad_ref, near_ref, x_high, x_low, kept, sent, g_high, g_low, t_high, t_low = refs

        @pl.when(pl.program_id(0) == 0)
        def _():
            frames, features = grad_ref.shape
            width = features // 4
            rows = width // 4
            padded = t_high.shape[1] // 2
            t_high[...] = jnp.zeros_like(t_high)
            t_low[...] = jnp.zeros_like(t_low)
            for clip in range(2):
                for dh in range(2):
                    if clip == 0:
                        part = grad_ref[:, 2 * dh * width : (2 * dh + 1) * width]
                    else:
                        part = near_ref[:, dh * width : (dh + 1) * width]
                    high, low = split(part.T)
                    at = (
                        slice(dh * width, (dh + 1) * width),
                        slice(clip * padded, clip * padded + frames),
                    )
                    t_high[at] = high
                    t_low[at] = low
            for group in range(8):
                first, second, dh = group // 4, group // 2 % 2, group % 2
                core = place_ref[6]
                y = place_ref[4] ^ (first * core + second * (1 - core))
                x = place_ref[5] ^ (first * (1 - core) + second * core)
                at = pl.multiple_of(dh * width + (2 * y + x) * rows, rows)
                g_high[group * rows : (group + 1) * rows, :] = t_high[pl.ds(at, rows), :]
                g_low[group * rows : (group + 1) * rows, :] = t_low[pl.ds(at, rows), :]

    else:
        g_high, g_low, x_high, x_low, kept, sent = refs
    half = g_high.shape[0] // 2
    value = product(g_high[...], g_low[...], x_high[...], x_low[...])
    kept[...] = value[:half].reshape(kept.shape)
    sent[...] = value[half:].reshape(sent.shape)


def weight_rows(side, place, grads, x_split, width):
    turn = side == 0
    whole = lambda array: pl.BlockSpec(array.shape, lambda s, place: (0,) * array.ndim)
    x_spec = pl.BlockSpec((x_split[0].shape[0], width), lambda s, place: (0, s))
    shape = (2, 2, width // 4, 4 * width)
    out_shape = [jax.ShapeDtypeStruct(shape, F32)] * 2
    out_specs = [pl.BlockSpec(shape[:3] + (width,), lambda s, place: (0, 0, 0, s))] * 2
    scratch = []
    if turn:
        turned = (2 * width, x_split[0].shape[0])
        out_shape += [jax.ShapeDtypeStruct(turned, BF16)] * 2
        out_specs += [whole(out_shape[-1])] * 2
        scratch = [pltpu.VMEM(turned, BF16)] * 2
    return call(
        partial(weight_body, turn),
        grid_spec=pltpu.PrefetchScalarGridSpec(
            num_scalar_prefetch=1,
            grid=(4,),
            in_specs=[whole(a) for a in grads] + [x_spec] * 2,
            out_specs=out_specs,
            scratch_shapes=scratch,
        ),
        out_shape=out_shape,
        hbm_outs=(0,),
        cost_estimate=cost(12 * x_split[0].shape[0] * width * 4 * width, 4 * 8 * width * width),
        name="weight_rows",
    )(place, *([in_hbm(grads[0]), grads[1]] if turn else grads), *[in_hbm(x) for x in x_split])


def step_body(n, widths, cut, *refs):
    ins, outs = refs[: 2 * n], refs[2 * n :]
    starts = [sum(widths[:i]) for i in range(len(widths))]
    column = 0
    for i in range(n):
        total = ins[2 * i][...] + ins[2 * i + 1][...]
        end = column + total.shape[-1]
        for j, (start, columns) in enumerate(zip(starts, widths)):
            low, high = max(start, column), min(start + columns, end)
            if low < high:
                to = (Ellipsis, slice(low - start, high - start))
                piece = total[..., low - column : high - column]
                pieces = [piece]
                for _ in range(cut):
                    pieces = [half[k] for half in pieces for k in range(2)]
                for k, some in enumerate(pieces):
                    outs[len(pieces) * j + k][to] = some
        column = end


def step_of(*pairs, cut=1, widths=None, hbm_outs=()):
    shape = list(pairs[0][0].shape)
    widths = widths or [sum(pair[0].shape[-1] for pair in pairs)]
    outs = []
    for columns in widths:
        shape[-1] = columns
        outs += [jax.ShapeDtypeStruct(tuple(shape[cut:]), F32)] * 2**cut
    whole = lambda array: pl.BlockSpec(array.shape, lambda i: (0,) * array.ndim)
    operands = [array for pair in pairs for array in pair]
    return call(
        partial(step_body, len(pairs), widths, cut),
        grid=(1,),
        in_specs=[whole(a) for a in operands],
        out_specs=[whole(a) for a in outs],
        out_shape=outs,
        hbm_outs=hbm_outs,
        cost_estimate=cost(0, 4 * sum(a.size for a in operands)),
        name="reduction_step",
    )(*operands)


def plane_swap(array, step):
    pairs = []
    for i in range(8):
        over_x = (i % 2 == 0) == (step == 0)
        pairs.append((i, i ^ 2 if over_x else i ^ 4))
    return lax.ppermute(array, ("y", "x", "c"), pairs)


def plane_gather(share, *before):
    first = plane_swap(share, 0)
    second = plane_swap(share, 1)
    return [share, second, first, plane_swap(after(first, second, *before), 1)]


def assemble_body(place_ref, *refs):
    out_ref = refs[-1]
    core = place_ref[6]
    rows, columns = refs[0].shape
    quarter = columns // 4
    for i in range(4):
        first, second = i // 2, i % 2
        y = place_ref[4] ^ (first * core + second * (1 - core))
        x = place_ref[5] ^ (first * (1 - core) + second * core)
        at = pl.multiple_of((2 * y + x) * rows, rows)
        for side in range(2):
            for h in range(2):
                to = pl.multiple_of((2 * h + (place_ref[7] ^ side)) * quarter, quarter)
                some = slice((2 * side + h) * quarter, (2 * side + h + 1) * quarter)
                out_ref[0, pl.ds(at, rows), pl.ds(to, quarter)] = refs[i][:, some]


def assemble(place, pieces, layer, onto=None):
    rows, columns = 4 * pieces[0].shape[0], pieces[0].shape[1]
    aliases, extra, extra_specs = {}, [], []
    if onto is not None:
        aliases, extra = {1 + len(pieces): 0}, [onto]
        extra_specs = [pl.BlockSpec(memory_space=pl.ANY)]
    (out,) = call(
        assemble_body,
        grid=(1,),
        out_shape=[jax.ShapeDtypeStruct((LAYERS, rows, columns), F32)],
        hbm_outs=(0,),
        in_specs=[SMEM_SPEC]
        + [pl.BlockSpec(p.shape, lambda i: (0, 0)) for p in pieces]
        + extra_specs,
        out_specs=[pl.BlockSpec((1, rows, columns), lambda i: (layer, 0, 0))],
        input_output_aliases=aliases,
        cost_estimate=cost(0, 8 * rows * columns),
        name="assemble",
    )(place, *[p if extra else in_hbm(p) for p in pieces], *extra)
    return out


def half_features(inputs, weights, gains, shifts, decays, biases, lengths, frame_mask, grad_out):
    width, slots = inputs.shape
    clips, frames = frame_mask.shape
    depth = weights.shape[2]
    blocks = 4 * width // LANES
    y, x, h, l, c = (lax.axis_index(name) for name in ("y", "x", "h", "l", "c"))
    b = 2 * y + x
    numbers = [2 * (h ^ (rel // 2)) + (c ^ (rel % 2)) for rel in range(4)] + [y, x, c, l]
    place = jnp.stack(numbers).astype(jnp.int32)
    own_blocks, other_blocks = (
        jnp.stack(
            [2 * (2 * (h ^ (rel // 2)) + half) + (c ^ (rel % 2)) for rel in range(4)]
        ).astype(jnp.int32)
        for half in (l, 1 - l)
    )
    own_columns = jnp.stack([2 * h + l, 2 * (1 - h) + l]).astype(jnp.int32)
    other_columns = jnp.stack([2 * (1 - h) + 1 - l, 2 * h + 1 - l]).astype(jnp.int32)
    rows = width // 4

    clip = 2 * h + c
    seen = lax.dynamic_index_in_dim(frame_mask, clip, 0, keepdims=False)
    length = lax.dynamic_index_in_dim(lengths, clip, 0, keepdims=False)
    moments = jnp.arange(frames, dtype=jnp.int32)
    gate = ((moments < length) & ((seen == 1) | (moments == 0))).astype(F32)
    valid = jnp.broadcast_to(gate[:, None], (frames, LANES))

    def far_share(layer):
        return lax.dynamic_slice(weights, (layer, b * rows, 0), (1, rows, depth))[0]

    def over_h(array):
        return lax.ppermute(array, "h", FLIP2)

    def over_c(array):
        return lax.ppermute(array, "c", FLIP2)

    def over_second(array):
        return plane_swap(array, 1)

    def four_of(near_rows, far_rows):
        return [
            (near_rows, 0),
            (over_c(near_rows), 1),
            (far_rows, 0),
            (over_c(far_rows), 1),
        ]

    def four_of_plane(share):
        both = lax.ppermute(share, ("y", "x"), DIAGONAL)
        return [share, lax.ppermute(share, "x", FLIP2), lax.ppermute(share, "y", FLIP2), both]

    near = over_c(weights)
    share = far_share(0)
    close, away = pack(place, after(inputs, share), frames)
    share = over_h(share)
    away = over_h(away)
    other_close = swap_half(close)
    up_close, up_away = pack(place, after(grad_out, close), frames, waits=True)
    share = after(share, up_close, valid, near)
    pieces = four_of_plane(share)
    away = after(away, pieces[1:], other_close)
    half_weights = [[weights, near, *pieces, *map(over_c, after(pieces, away))]]
    own = four_of(after(close, away), away)
    other_away = swap_half(away)
    others = [(other_close, 0), (over_c(other_close), 1)]
    params = jnp.stack([gains, shifts + biases, decays], axis=1)
    own_params = params.reshape(LAYERS * 3 * width // LANES, LANES)
    params = None

    def gather(array, axes):
        return lax.all_gather(array, axes, tiled=True)

    weight = half_weights[0]
    early = jnp.concatenate([own_blocks, other_blocks[:2]])
    z, own_flat = project(place, frames, own + others, early, weight, 0, flat=own)
    others += [(other_away, 0), (over_c(after(other_away, z)[frames:]), 0)]
    z, stats, other_flat = project(
        place,
        frames,
        others[2:],
        other_blocks[2:],
        weight,
        0,
        z,
        valid,
        params=own_params,
        flat=others,
    )
    z = [z]
    stats = gather(stats, ("h", "c"))
    share = over_c(lax.ppermute(after(far_share(1), stats), ("h", "c"), DIAGONAL))
    stats = gather(stats, ("y", "x"))
    x, states, slopes, params = recur(0, place, gate, z, stats, None, valid, own_flat, False)
    own_near, other_near = over_c(after(own_flat, z[0])), over_c(after(other_flat, z[0]))
    x_near = over_c(x)
    own_split = prepare(place, after(own_flat, x_near), own_near)
    other_split = prepare(place, after(other_flat, x_near), other_near)
    saved = [(own_split, other_split, z, stats, states, slopes)]

    pieces = four_of_plane(after(share, slopes, own_near, other_near))
    near = [weights, near]
    other = swap_half(x)
    x_own = after(x, own_split[0], other_split[0])
    z, *_ = project(place, frames, [(x_own, None)], own_blocks, near, 1)
    own_split = prepare(place, after(x, z), x_near)
    far = [*pieces, *map(over_c, after(pieces, own_split[0]))]
    up_away = over_h(after(up_away, own_split[0]))
    half_weights.append(near + far)
    z, stats = project(place, frames, [(other, None)], other_blocks, near, 1, z, valid)
    both = jnp.concatenate([own_blocks, other_blocks])
    z_far, stats = project(
        place,
        frames,
        [(x, None), (other, None)],
        both,
        far,
        1,
        None,
        valid,
        stats,
    )
    z = [z, z_far]
    stats = gather(gather(stats, ("y", "x")), ("h", "c"))
    upstream = four_of(up_close, after(up_away, stats))
    *output, states, slopes = recur(1, place, gate, z, stats, params, valid, x, True)
    other_near = over_c(after(other, slopes))
    saved.append((own_split, (other, other_near), z, stats, states, slopes))
    diagonal = over_c(over_h(output[3]))

    ups = upstream
    results = [None] * LAYERS
    for layer in range(LAYERS - 1, -1, -1):
        own_split, other_split, z, stats, states, slopes = saved[layer]
        weight = half_weights[layer]
        grad_pre, sums = back(layer, place, gate, z, stats, params, ups, states, slopes)
        sums = gather(sums, ("y", "x"))
        if layer == 0:
            come[0] = after(come[0], sums, away, output[1][0])
            later, go = step_of((in_hbm(stay[0]), come[0]), (in_hbm(stay[1]), come[1]))
            sums = after(sums, later)
            go = over_second(go)
        sums = gather(sums, ("h", "c"))
        grad_z, leaving, *terms, sums = norm_back(
            other_columns, place, grad_pre, z, params, valid, stats, sums, weight, layer,
            layer == 0,
        )
        leaving = over_c(leaving)
        if layer > 0:
            received = [swap_half(terms[0])]
            other_split = prepare(place, *after(other_split, grad_z))
            leaving = after(leaving, diagonal, other_split[0])
        else:
            received = [None, swap_half(terms[1])]
            later, go = step_of((later, after(go, grad_z)), hbm_outs=(0,))
            leaving = after(leaving, later)
            go = lax.ppermute(go, ("h", "c"), DIAGONAL)
            later = (later, go)
        *first, g_high, g_low = weight_rows(0, place, (grad_z, leaving), own_split, width)
        turned = (g_high, g_low)
        come = [plane_swap(first[1], 0)]
        if layer == 0:
            received[0] = swap_half(after(terms[0], received[1]))
        second = weight_rows(1, place, turned, other_split, width)
        come.append(plane_swap(second[1], 0))
        stay = (first[0], second[0])
        kept = own_terms(own_columns, place, after(grad_z, second[0]), ups, weight, layer)
        if layer > 0:
            away = over_h(after(output[2], kept))
            output = [(a, 0) for a in (output[0], over_c(output[1]), away, diagonal)]
        ups = [(kept, None)] + [(r, None) for r in received]
        results[layer] = lax.dynamic_index_in_dim(
            sums.reshape(3, 4, width), clip, axis=1, keepdims=False
        )

    sums = jnp.stack(results)
    sums = [sums[:, 0], sums[:, 1], sums[:, 2]]
    sums.append(jnp.stack(after(results, kept))[:, 1])
    aways = merge(kept, 1, received[1], apart=True)
    later = (in_hbm(later[0]), over_c(after(later[1], aways[0])))
    (later,) = step_of(later, cut=0, hbm_outs=(0,))
    come[0] = after(come[0], sums, later)
    far_near = over_c(lax.ppermute(aways[0], ("h", "c"), DIAGONAL))
    near_sum, far_sum, near_go, far_go = step_of(
        (in_hbm(stay[0]), come[0]), (in_hbm(stay[1]), come[1]), cut=2
    )
    near_go, far_go = over_second(near_go), over_second(far_go)
    (go,) = step_of((far_sum, after(far_go, far_near)), cut=0)
    later = after(later, go)
    go = over_h(go)
    later = plane_gather(later)
    (total,) = step_of((near_sum, near_go), cut=0)
    output = unpack(place, [(after(array, total), i) for array, i in output], frames, waited=True)
    close = merge(kept, 0, after(received[0], output))
    far = over_c(over_h(after(aways[1], go)))
    (share,) = step_of((total, after(go, close, *later[1:])), cut=0)
    grad_weights = assemble(place, after(later, share), 1)
    gathered = plane_gather(share, grad_weights)
    grad_in = [(close, 0), (over_c(close[frames:]), 0), (far_near, 0), (far, 0)]
    grad_in = unpack(place, grad_in, frames)
    grad_weights = assemble(place, after(gathered, grad_in), 0, grad_weights)
    return (output, grad_in, grad_weights, *sums)


def gelu_slope(value):
    return (
        0.5 * (1.0 + jax.scipy.special.erf(value / ROOT_TWO))
        + value * jnp.exp(-0.5 * value * value) / ROOT_TWO_PI
    )


def recur_step(decay, state, inputs):
    drive_t, valid_t = inputs
    pre = drive_t + decay * state
    state = state + valid_t * (jax.nn.gelu(pre, approximate=False) - state)
    return (state, state)


def back_step(decay, carry, inputs):
    upstream_t, valid_t, pre_t = inputs
    total = upstream_t + carry
    grad_pre = total * valid_t * gelu_slope(pre_t)
    carry = total * (1.0 - valid_t) + grad_pre * decay
    return (carry, grad_pre)


def add_piece(weight, piece):
    return jnp.dot(weight, piece, precision=HIGH, preferred_element_type=jnp.float32)


def weight_columns(grad_pre_norm, piece):
    return jnp.einsum("jf,kf->jk", grad_pre_norm, piece, precision=HIGH)


def split_features(inputs, weights, gains, shifts, decays, biases, lengths, frame_mask, grad_out):
    width, slots = inputs.shape
    clips, frames_len = frame_mask.shape
    frames = jnp.arange(frames_len, dtype=jnp.int32)
    valid_grid = (
        (frames[None, :] < lengths[:, None]) & ((frame_mask == 1) | (frames[None, :] == 0))
    ).astype(jnp.float32)
    valid = valid_grid.reshape(-1)
    valid_row = valid[None, :]
    valid_time = jnp.broadcast_to(valid_grid.T[:, :, None], (frames_len, clips, width)).reshape(
        frames_len, clips * width
    )
    count_local = jnp.sum(valid)

    def to_time(array):
        return jnp.transpose(array.reshape(width, clips, frames_len), (2, 1, 0)).reshape(
            frames_len, clips * width
        )

    def from_time(array):
        return jnp.transpose(array.reshape(frames_len, clips, width), (2, 1, 0)).reshape(
            width, slots
        )

    layer_in = inputs
    saved = []
    for layer_no in range(LAYERS):
        weight = weights[layer_no]
        gathered = lax.all_gather(layer_in, "neuron", axis=0, tiled=True)
        pre_norm = add_piece(weight, gathered)
        first_sum, count = lax.psum((jnp.sum(valid_row * pre_norm, axis=1), count_local), "batch")
        mean = first_sum / count
        centered = pre_norm - mean[:, None]
        var = lax.psum(jnp.sum(valid_row * centered * centered, axis=1), "batch") / count
        inv_std = lax.rsqrt(var + EPS)
        zhat = (pre_norm - mean[:, None]) * inv_std[:, None]
        drive = gains[layer_no][:, None] * zhat + (shifts[layer_no] + biases[layer_no])[:, None]
        drive_time = to_time(drive)
        decay_wide = jnp.tile(decays[layer_no], clips)
        start_state = jnp.zeros((clips * width,), jnp.float32)
        _, states = lax.scan(
            partial(recur_step, decay_wide), start_state, (drive_time, valid_time), unroll=8
        )
        saved.append((gathered, zhat, inv_std, drive_time, states, count))
        layer_in = layer_in + valid_row * from_time(states)
    upstream = grad_out
    grad_parts = [None] * LAYERS
    for layer_no in range(LAYERS - 1, -1, -1):
        gathered, zhat, inv_std, drive_time, states, count = saved[layer_no]
        decay_wide = jnp.tile(decays[layer_no], clips)
        gain = gains[layer_no]
        previous = jnp.concatenate([jnp.zeros_like(states[:1]), states[:-1]], axis=0)
        pre_time = drive_time + decay_wide[None, :] * previous
        grad_state = to_time(valid_row * upstream)
        start_carry = jnp.zeros((clips * width,), jnp.float32)
        _, grad_pre_time = lax.scan(
            partial(back_step, decay_wide),
            start_carry,
            (grad_state, valid_time, pre_time),
            reverse=True,
            unroll=8,
        )
        decay_local = jnp.sum(
            jnp.sum(grad_pre_time * previous, axis=0).reshape(clips, width), axis=0
        )
        grad_pre = from_time(grad_pre_time)
        gain_local = jnp.sum(grad_pre * zhat, axis=1)
        shift_local = jnp.sum(grad_pre, axis=1)
        grad_gain, grad_shift, grad_decay = lax.psum(
            (gain_local, shift_local, decay_local), "batch"
        )
        grad_pre_norm = (gain * inv_std)[:, None] * (
            grad_pre - valid_row * (grad_shift[:, None] + zhat * grad_gain[:, None]) / count
        )
        weight_local = weight_columns(grad_pre_norm, gathered)
        input_terms = jnp.einsum("jk,jf->kf", weights[layer_no], grad_pre_norm, precision=HIGH)
        input_grad = lax.psum_scatter(input_terms, "neuron", scatter_dimension=0, tiled=True)
        grad_weight = lax.psum(weight_local, "batch")
        upstream = upstream + input_grad
        grad_parts[layer_no] = (grad_weight, grad_gain, grad_shift, grad_decay)
    grad_weights = jnp.stack([grad_parts[layer_no][0] for layer_no in range(LAYERS)])
    grad_gains = jnp.stack([grad_parts[layer_no][1] for layer_no in range(LAYERS)])
    grad_shifts = jnp.stack([grad_parts[layer_no][2] for layer_no in range(LAYERS)])
    grad_decays = jnp.stack([grad_parts[layer_no][3] for layer_no in range(LAYERS)])
    return (layer_in, upstream, grad_weights, grad_gains, grad_shifts, grad_decays, grad_shifts)


def solution(mesh):
    if (mesh.shape["batch"], mesh.shape["neuron"]) == (4, 8):
        cut = Mesh(mesh.devices.reshape(2, 2, 2, 2, 2), ("y", "x", "h", "l", "c"))
        batch, neuron, body = ("y", "x"), ("h", "l", "c"), half_features
    else:
        cut, batch, neuron, body = mesh, "batch", "neuron", split_features
    in_specs = (
        P(neuron, batch),
        P(None, neuron, None),
        P(None, neuron),
        P(None, neuron),
        P(None, neuron),
        P(None, neuron),
        P(batch),
        P(batch, None),
        P(neuron, batch),
    )
    out_specs = (
        P(neuron, batch),
        P(neuron, batch),
        P(None, neuron, None),
        P(None, neuron),
        P(None, neuron),
        P(None, neuron),
        P(None, neuron),
    )
    return jax.shard_map(
        body, mesh=cut, in_specs=in_specs, out_specs=out_specs, check_vma=False
    )
```
